32 devices in a mesh: nodes: 8 (over z, x), rep: 4 (over y, core).
Axes of the slice: x: 2, y: 2, z: 4, core: 2. Of those that a mesh axis runs over, the one named last changes fastest.
Arguments:
- node_input: bfloat16 [6144, 256], P(('rep', 'nodes')), may hold values from -16 to 16
- edge_feat: bfloat16 [12288, 256], P(('rep', 'nodes')), may hold values from -6 to 6
- graph_ids: int32 [6144], P(('rep', 'nodes')), may hold values from 0 to 1536, as said below
- edge_src: int32 [12288], P(('rep', 'nodes')), may hold values from 0 to 239, as said below
- edge_dst: int32 [12288], P(('rep', 'nodes')), may hold values from 0 to 191, as said below
- halo_send: int32 [1536], P(('rep', 'nodes')), may hold values from 0 to 191, as said below
- w_proj: bfloat16 [2, 256, 1024], replicated, may hold values from -0.375 to 0.375
- w_edge: bfloat16 [2, 256, 256], replicated, may hold values from -0.375 to 0.375
- w_qkv: bfloat16 [2, 256, 768], replicated, may hold values from -0.25 to 0.25
- w_out: bfloat16 [2, 256, 256], replicated, may hold values from -1.5 to 1.5
- w_up: bfloat16 [2, 256, 512], replicated, may hold values from -0.375 to 0.375
- w_down: bfloat16 [2, 512, 256], replicated, may hold values from -0.25 to 0.25
- norm_gain: float32 [2, 3, 256], replicated, may hold values from 0.5 to 1.5
- norm_shift: float32 [2, 3, 256], replicated, may hold values from -1.5 to 1.5
- cotangent: bfloat16 [6144, 256], P(('rep', 'nodes')), may hold values from -6 to 6
Outputs:
- out_act: float32 [6144, 256], P(('rep', 'nodes'))
- grad_input: float32 [6144, 256], P(('rep', 'nodes'))
- grad_proj: float32 [2, 256, 1024], replicated
- grad_edge: float32 [2, 256, 256], replicated
- grad_qkv: float32 [2, 256, 768], replicated
- grad_out: float32 [2, 256, 256], replicated
- grad_up: float32 [2, 256, 512], replicated
- grad_down: float32 [2, 512, 256], replicated
- grad_gain: float32 [2, 3, 256], replicated
- grad_shift: float32 [2, 3, 256], replicated
The draws below stay inside these ranges and needn't reach their ends.
Inputs may be any that keep to these rules, and one draw needn't show every extreme that they name: `graph_ids`: nodes of one group attend to each other only where their graph ids are equal; ids of different groups are unrelated. `edge_src`: indexes the device's 192 nodes followed by the 24 rows received from the previous and the 24 rows from the next device along nodes; every one of these rows is the source of some edge. `edge_dst`: every node of a device is the target of at least one of its edges. `halo_send`: per device, 24 distinct rows for the previous neighbour, then 24 distinct rows for the next.
All inputs are finite; a program needn't handle non-finite values.
Results may differ from the reference program's by a relative error of at most 0.025.
Values may be sent and summed in bfloat16 or wider, within the bound.
A program may use at most 256 MiB of HBM per device.

```python
import math
import jax
import jax.numpy as jnp
from jax import lax

HEADS = 8
HEAD_DIM = 32
D = 256
FF = 512
LAYERS = 2
NDEV = 192
HALO = 24
GROUP = 1536
NODES = 6144
EDGES = 12288
SENDS = 1536
N_NODES = 8
N_REP = 4


def shuffle_rows(key, row_total, length):
    row_keys = jax.random.split(key, row_total)

    def one_row(row_key):
        return jax.random.permutation(row_key, length)
    return jax.vmap(one_row)(row_keys)


def draw_node_input(key, part):
    key = jax.random.fold_in(key, 1)
    noise_key, common_key = jax.random.split(key)
    position = jnp.arange(NODES, dtype=jnp.float32)[:, None] / NODES
    common = jnp.clip(jax.random.normal(common_key, (1, D), jnp.float32), -1.5, 1.5)
    rising = 0.7 + 1.4 * position
    noise_draw = jnp.clip(jax.random.normal(noise_key, (NODES, D), jnp.float32), -4.0, 4.0)
    return ((noise_draw + 0.5 * common) * rising).astype(jnp.bfloat16)


def draw_graph_ids(key, part):
    key = jax.random.fold_in(key, 7)
    devices_all = N_NODES * N_REP
    level_key, wide_key, forced_key, open_key = jax.random.split(key, 4)
    levels = jax.random.randint(level_key, (devices_all, 1), 1, 5)
    in_wide = jax.random.randint(wide_key, (devices_all, NDEV), 0, 8) < levels
    forced = jax.random.randint(forced_key, (devices_all, 1), 0, NDEV - 1)
    in_wide = in_wide | (jnp.arange(NDEV, dtype=jnp.int32)[None, :] == forced)
    in_wide = in_wide.reshape(N_REP, GROUP)
    position = jnp.arange(GROUP, dtype=jnp.int32)[None, :]
    is_last = position == GROUP - 1
    in_wide = in_wide & jnp.logical_not(is_last)
    opens = (jax.random.randint(open_key, (devices_all, NDEV), 0, 12) == 0).reshape(N_REP, GROUP)
    opens = (opens | is_last) & jnp.logical_not(in_wide)
    starts = jnp.where(opens, position, 0).astype(jnp.int32)
    small_ids = 1 + lax.cummax(starts, axis=1)
    graph_ids = jnp.where(in_wide, 0, small_ids)
    return graph_ids.reshape(NODES).astype(jnp.int32)


def edge_indices(key, reach_rows):
    devices_all = N_NODES * N_REP
    first_key, second_key, third_key = jax.random.split(key, 3)
    covered = shuffle_rows(first_key, devices_all, reach_rows)
    extra_rows = jax.random.randint(second_key, (devices_all, 2 * NDEV - reach_rows), 0, reach_rows)
    joined = jnp.concatenate([covered, extra_rows], 1)
    shuffle_order = shuffle_rows(third_key, devices_all, 2 * NDEV)
    return jnp.take_along_axis(joined, shuffle_order, 1).reshape(EDGES).astype(jnp.int32)


def draw_edge_src(key, part):
    key = jax.random.fold_in(key, 11)
    return edge_indices(key, NDEV + 2 * HALO)


def draw_edge_dst(key, part):
    key = jax.random.fold_in(key, 12)
    return edge_indices(key, NDEV)


def draw_halo_send(key, part):
    key = jax.random.fold_in(key, 13)
    picks = shuffle_rows(key, 2 * N_NODES * N_REP, NDEV)[:, :HALO]
    return picks.reshape(SENDS).astype(jnp.int32)


def raised(array, own_key, source, target, parts, factor):
    owner, partner = [(jnp.arange(array.shape[dim]) // (array.shape[dim] // parts)).reshape([-1 if axis == dim else 1 for axis in range(array.ndim)]) for dim in (source, target)]
    chosen = jax.random.permutation(own_key, parts)[partner]
    strong = (owner == chosen) | (owner == (partner + parts // 2) % parts)
    return jnp.where(strong, factor * array, array)


def steps_of(stream_key, shape, cuts, least, largest):
    def one(axis_at, blocks):
        heights = jax.random.uniform(jax.random.fold_in(jax.random.fold_in(stream_key, 6), axis_at), (blocks,), jnp.float32, least / len(cuts), largest / len(cuts))
        return jnp.repeat(jnp.exp(heights), shape[axis_at] // blocks).reshape((-1,) + (1,) * (len(shape) - axis_at - 1))

    factor_of = one(*cuts[0])
    for cut in cuts[1:]:
        factor_of = factor_of * one(*cut)
    return factor_of


def scatter_about(own_key, extent, deviation, limit, cuts=(), kind=jnp.bfloat16):
    array = jax.random.normal(own_key, extent, jnp.float32) * deviation
    if len(cuts) > 0:
        array = steps_of(own_key, extent, cuts, -0.22, 0.18) * array
    return jnp.clip(array, min=-limit, max=limit).astype(kind)


def bell_draw_with(stream_key, shape, width, bound, cuts, heavy, held_as=jnp.bfloat16):
    values = width * jax.random.normal(stream_key, shape, jnp.float32)
    if cuts:
        values = values * steps_of(stream_key, shape, cuts, -0.22, 0.18)
    return jnp.clip(raised(values, jax.random.fold_in(stream_key, 3), *heavy), -bound, bound).astype(held_as)


def setup_inputs(seed: int = 0) -> dict:
    splits = jax.random.split(jax.random.key(seed), 16)
    node_input = draw_node_input(jax.random.fold_in(splits[15], 71), 0)
    edge_feat = scatter_about(splits[1], (EDGES, D), 1.0, 6.0, ((0, 32),))
    graph_ids = draw_graph_ids(jax.random.fold_in(splits[15], 71), 0)
    edge_src = draw_edge_src(jax.random.fold_in(splits[15], 71), 0)
    edge_dst = draw_edge_dst(jax.random.fold_in(splits[15], 71), 0)
    halo_send = draw_halo_send(jax.random.fold_in(splits[15], 71), 0)
    w_proj = scatter_about(splits[6], (LAYERS, D, 4 * D), D ** -0.5, 0.375)
    w_edge = scatter_about(splits[7], (LAYERS, D, D), D ** -0.5, 0.375)
    w_qkv = scatter_about(splits[8], (LAYERS, D, 3 * D), (2 * D) ** -0.5, 0.25)
    w_out = scatter_about(splits[9], (LAYERS, D, D), (D // 16) ** -0.5, 1.5)
    w_up = scatter_about(splits[10], (LAYERS, D, FF), D ** -0.5, 0.375)
    w_down = scatter_about(splits[11], (LAYERS, FF, D), FF ** -0.5, 0.25)
    norm_gain = jnp.clip(1.0 + 0.1 * jax.random.normal(splits[12], (LAYERS, 3, D), jnp.float32), 0.5, 1.5)
    norm_shift = scatter_about(splits[13], (LAYERS, 3, D), 0.3, 1.5, (), jnp.float32)
    cotangent = bell_draw_with(splits[14], (NODES, D), 1.0, 6.0, ((0, 32),), (0, 1, 32, 2.75))
    return {"node_input": node_input, "edge_feat": edge_feat, "graph_ids": graph_ids, "edge_src": edge_src, "edge_dst": edge_dst, "halo_send": halo_send, "w_proj": w_proj, "w_edge": w_edge, "w_qkv": w_qkv, "w_out": w_out, "w_up": w_up, "w_down": w_down, "norm_gain": norm_gain, "norm_shift": norm_shift, "cotangent": cotangent}


@jax.custom_vjp
def low(v):
    return lax.optimization_barrier(v.astype(jnp.bfloat16)).astype(jnp.float32)

@jax.custom_vjp
def low_back(v):
    return v

def low_keep(v):
    return (low(v), None)

def low_pass(kept, grad):
    return (grad,)

def back_keep(v):
    return (v, None)

def back_low(kept, grad):
    return (low(grad),)
low.defvjp(low_keep, low_pass)
low_back.defvjp(back_keep, back_low)
HIGH = lax.Precision.HIGHEST
NEG = -1e+30

def matmul(left, right):
    return jnp.dot(left, right, precision=HIGH, preferred_element_type=jnp.float32)

def batch_norm(inputs, gains, shifts):
    batch_mean = lax.optimization_barrier(jnp.mean(inputs, 0))
    batch_var = lax.optimization_barrier(jnp.mean((inputs - batch_mean) ** 2, 0))
    return (inputs - batch_mean) * lax.rsqrt(batch_var + 1e-05) * gains + shifts

def group_attention(group_args):
    query_rows, key_rows, value_rows, group_graphs = group_args
    block_rows = math.gcd(GROUP, 512)
    query_blocks = query_rows.reshape(GROUP // block_rows, block_rows, HEADS, HEAD_DIM)
    query_graphs = group_graphs.reshape(GROUP // block_rows, block_rows)
    key_heads = key_rows.reshape(GROUP, HEADS, HEAD_DIM)
    value_heads = value_rows.reshape(GROUP, HEADS, HEAD_DIM)

    def one_block(block_pair):
        query_block, block_graphs = block_pair
        scores = jnp.einsum('qhd,khd->hqk', query_block, key_heads, precision=HIGH) / math.sqrt(HEAD_DIM)
        scores = low_back(scores)
        same_graph = (block_graphs[:, None] == group_graphs[None, :])[None]
        scores = jnp.where(same_graph, scores, NEG)
        row_max = lax.optimization_barrier(jnp.max(scores, 2, keepdims=True))
        raw_weights = jnp.exp(scores - row_max)
        attn_weights = raw_weights / lax.optimization_barrier(jnp.sum(raw_weights, 2, keepdims=True))
        return jnp.einsum('hqk,khd->qhd', low(attn_weights), value_heads, precision=HIGH)
    result = lax.map(jax.checkpoint(one_block), (query_blocks, query_graphs))
    return result.reshape(GROUP, HEADS * HEAD_DIM)

def global_sources(edge_src, halo_send):
    device = jnp.arange(EDGES, dtype=jnp.int32) // (2 * NDEV)
    column = device % N_NODES
    group_base = device - column
    prev_dev = group_base + (column + N_NODES - 1) % N_NODES
    next_dev = group_base + (column + 1) % N_NODES
    send_rows = halo_send.reshape(N_NODES * N_REP, 2 * HALO)
    from_prev = send_rows[prev_dev, jnp.clip(edge_src - NDEV + HALO, 0, 2 * HALO - 1)]
    from_next = send_rows[next_dev, jnp.clip(edge_src - NDEV - HALO, 0, 2 * HALO - 1)]
    local_index = device * NDEV + edge_src
    remote = jnp.where(edge_src < NDEV + HALO, prev_dev * NDEV + from_prev, next_dev * NDEV + from_next)
    return jnp.where(edge_src < NDEV, local_index, remote).astype(jnp.int32)

def layer(hidden, params, edge_values, sources, targets, graph_ids):
    w_proj, w_edge, w_qkv, w_out, w_up, w_down, norm_gains, norm_shifts = params
    hidden_low = low(hidden)
    projected = low_back(matmul(hidden_low, w_proj))
    self_term = projected[:, :D]
    source_b = low(projected[:, D:2 * D])
    dest_term = projected[:, 2 * D:3 * D]
    source_e = low(projected[:, 3 * D:])
    edge_proj = low_back(matmul(edge_values, w_edge))
    gating = jax.nn.sigmoid(dest_term[targets] + source_e[sources] + edge_proj)
    numerator = jax.ops.segment_sum(gating * source_b[sources], targets, NODES)
    denominator = jax.ops.segment_sum(gating, targets, NODES)
    message = self_term + numerator / (denominator + 1e-06)
    local_out = hidden + jax.nn.silu(batch_norm(message, norm_gains[0], norm_shifts[0]))
    qkv_low = low_back(low(matmul(hidden_low, w_qkv)))
    query_rows = qkv_low[:, :D].reshape(N_REP, GROUP, D)
    key_rows = qkv_low[:, D:2 * D].reshape(N_REP, GROUP, D)
    value_rows = qkv_low[:, 2 * D:].reshape(N_REP, GROUP, D)
    attended = lax.map(jax.checkpoint(group_attention), (query_rows, key_rows, value_rows, graph_ids.reshape(N_REP, GROUP)))
    attn_low = low_back(low(attended.reshape(NODES, D)))
    attn_proj = low_back(matmul(attn_low, w_out))
    attn_out = batch_norm(hidden + attn_proj, norm_gains[1], norm_shifts[1])
    mixed = local_out + attn_out
    up_proj = low_back(matmul(low(mixed), w_up))
    down_proj = low_back(matmul(low(jax.nn.silu(up_proj)), w_down))
    return batch_norm(mixed + down_proj, norm_gains[2], norm_shifts[2])

def reference(node_input, edge_feat, graph_ids, edge_src, edge_dst, halo_send, w_proj, w_edge, w_qkv, w_out, w_up, w_down, norm_gain, norm_shift, cotangent):
    sources = global_sources(edge_src, halo_send)
    targets = (jnp.arange(EDGES, dtype=jnp.int32) // (2 * NDEV) * NDEV + edge_dst).astype(jnp.int32)
    edge_values = edge_feat.astype(jnp.float32)

    def forward(hidden, proj_all, edge_all, qkv_all, out_all, up_all, down_all, gain_all, shift_all):
        for layer_index in range(LAYERS):
            params = (proj_all[layer_index], edge_all[layer_index], qkv_all[layer_index], out_all[layer_index], up_all[layer_index], down_all[layer_index], gain_all[layer_index], shift_all[layer_index])
            hidden = layer(hidden, params, edge_values, sources, targets, graph_ids)
        return hidden
    result, pullback = jax.vjp(forward, node_input.astype(jnp.float32), w_proj.astype(jnp.float32), w_edge.astype(jnp.float32), w_qkv.astype(jnp.float32), w_out.astype(jnp.float32), w_up.astype(jnp.float32), w_down.astype(jnp.float32), norm_gain, norm_shift)
    gradients = pullback(cotangent.astype(jnp.float32))
    return (result, gradients[0], gradients[1], gradients[2], gradients[3], gradients[4], gradients[5], gradients[6], gradients[7], gradients[8])
```

```python
import functools
import math

import jax
import jax.numpy as jnp
from jax import lax
from jax.experimental import pallas as pl
from jax.experimental.pallas import tpu as pltpu
from jax.sharding import PartitionSpec as P

HEADS = 8
HEAD_DIM = 32
NEG = -1e30
NORM_EPS = 1e-05
GATE_EPS = 1e-06
F32, BF16, I32 = jnp.float32, jnp.bfloat16, jnp.int32
MESH = pl.DeviceIdType.MESH
SYNCS = 7


def dot(left, right):
    return lax.dot_general(
        left, right, (((1,), (0,)), ((), ())), preferred_element_type=F32
    )


def dot_nt(left, right):
    return lax.dot_general(
        left, right, (((1,), (1,)), ((), ())), preferred_element_type=F32
    )


def dot_tn(left, right):
    return lax.dot_general(
        left, right, (((0,), (0,)), ((), ())), preferred_element_type=F32
    )


def split(value):
    high = value.astype(BF16)
    return high, (value - high.astype(F32)).astype(BF16)


def select_rows(onehot, value):
    high, low = split(value)
    return dot(onehot, high) + dot(onehot, low)


def sigmoid(value):
    return 1.0 / (1.0 + jnp.exp(-value))


def silu_slope(value):
    logistic = sigmoid(value)
    return logistic * (1.0 + value * (1.0 - logistic))


def col_sum(value):
    return jnp.sum(value, axis=0, keepdims=True)


def pack(first, second, third, fourth):
    halves = []
    for row in (first, second, third, fourth):
        halves += [row[:, :128], row[:, 128:]]
    return jnp.concatenate(halves, 0)


def unpack(tile):
    return [
        jnp.concatenate([tile[2 * i : 2 * i + 1], tile[2 * i + 1 : 2 * i + 2]], 1)
        for i in range(4)
    ]


def combine_pair(tiles, count):
    mean = jnp.mean(tiles[:, 0:4], 0)
    off = tiles[:, 0:4] - mean
    return jnp.concatenate([mean, jnp.sum(tiles[:, 4:8] + count * off * off, 0)], 0)


def combine_last(tiles, count):
    mean = jnp.mean(tiles[:, 0:2], 0)
    off = tiles[:, 0:2] - mean
    return jnp.concatenate(
        [
            mean,
            jnp.sum(tiles[:, 2:4], 0),
            jnp.sum(tiles[:, 4:6] + count * off * off, 0),
            jnp.sum(tiles[:, 6:8] + off * tiles[:, 2:4], 0),
        ],
        0,
    )


def combine_sum(tiles, count):
    return jnp.sum(tiles, 0)


class Refs:
    pass


def scratch_list(N, M, L, R, E):
    NZ, G, HR = N // 2, N * R, HEADS * R
    D, FF = 256, 512
    late, early = 2048, 2560
    dma = lambda *shape: pltpu.SemaphoreType.DMA(shape)
    vm = lambda dtype, *shape: pltpu.VMEM(shape, dtype)
    names = dict(
        xs=vm(BF16, L, N, R, D),
        yc=vm(BF16, N, R, D),
        meta=vm(I32, N, 8, 256),
        st1=vm(F32, SYNCS, N, 8, 128),
        st2=vm(F32, SYNCS, M, 8, 128),
        T=vm(BF16, E, R),
        TT=vm(BF16, R, E),
        S=vm(BF16, E, 256),
        ST=vm(BF16, 256, E),
        efT=vm(BF16, D, E),
        HP=vm(BF16, 32, R),
        HN=vm(BF16, 32, R),
        A=vm(BF16, R, 64),
        bias=vm(F32, R, G),
        ce=vm(F32, L, E, D),
        xf=vm(F32, L, R, D),
        xe=vm(BF16, L, 256, D),
        gate=vm(F32, L, E, D),
        bs=vm(BF16, L, E, D),
        num=vm(F32, L, R, D),
        den=vm(F32, L, R, D),
        z0=vm(F32, L, R, D),
        z1=vm(F32, L, R, D),
        z2=vm(F32, L, R, D),
        q=vm(F32, L, R, D),
        kk=vm(BF16, L, G, D),
        vv=vm(BF16, L, G, D),
        pst=vm(BF16, L, HR, G),
        oraw=vm(F32, L, R, D),
        inv=vm(F32, L, R, D),
        ob=vm(BF16, L, R, D),
        mb=vm(BF16, L, R, D),
        u=vm(F32, L, R, FF),
        g=vm(BF16, L, R, FF),
        iv=vm(F32, L, 8, D),
        dmix=vm(F32, R, D),
        dxo=vm(F32, R, D),
        qm=vm(BF16, HR, D),
        qmT=vm(BF16, D, HR),
        dom=vm(BF16, HR, D),
        domT=vm(BF16, D, HR),
        delta=vm(F32, HR, 1),
        dss=vm(BF16, HR, G),
        gkv=vm(F32, 2 * D, D),
        dxs=vm(BF16, L, NZ, 2, R, D),
        rs1=vm(BF16, L, NZ, R, D),
        cs=vm(BF16, L, NZ, R, D),
        rs2=vm(BF16, L, NZ, R, D),
        hs=vm(BF16, L, 2, 32, D),
        hr=vm(BF16, L, 2, 32, D),
    )
    for g, rows in enumerate((late, early, late)):
        names[f"gs{g}"] = vm(BF16, rows, D)
        names[f"a1_{g}"] = vm(BF16, M, rows // M, D)
        names[f"gt{g}"] = vm(BF16, rows // M, D)
        names[f"a2_{g}"] = vm(BF16, N, rows // (M * N), D)
    names.update(
        meta_s=dma(N),
        meta_r=dma(N),
        st1_s=dma(SYNCS, N),
        st1_r=dma(SYNCS, N),
        st2_s=dma(SYNCS, M),
        st2_r=dma(SYNCS, M),
        agc_s=dma(L, NZ),
        agc_r=dma(L, NZ),
        agp_s=dma(L, NZ),
        agp_r=dma(L, NZ),
        rsp_s=dma(L, NZ),
        rsp_r=dma(L, NZ),
        rsc_s=dma(L, NZ),
        rsc_r=dma(L, NZ),
        hal_s=dma(L, 2),
        hal_r=dma(L, 2),
        ar_s=dma(3, 4, max(N, M)),
        ar_r=dma(3, 4, max(N, M)),
    )
    return names


IN_NAMES = (
    "x_in", "meta_in", "edges", "ef", "wp", "we", "wqkv", "wo", "wu", "wd",
    "gain", "shift", "cot",
)
OUT_NAMES = ("out_act", "grad_in", "gout0", "gout1", "gout2", "ggain", "gshift")


def kernel(N, M, L, names, *args):
    r_ = Refs()
    for name, ref in zip(IN_NAMES + OUT_NAMES + tuple(names), args, strict=True):
        setattr(r_, name, ref)
    R, D = r_.x_in.shape
    E = r_.ef.shape[0]
    FF = 512
    NZ, G, HR = N // 2, N * R, HEADS * R
    total = float(N * M * R)
    scale = HEAD_DIM ** -0.5
    me = lax.axis_index("nodes")
    rep = lax.axis_index("rep")
    z = me // 2
    par = me % 2
    partner = 2 * z + (1 - par)
    prev = (me + N - 1) % N
    nxt = (me + 1) % N
    pending = []

    def remote(src, dst, s_sem, r_sem, **where):
        return pltpu.make_async_remote_copy(
            src_ref=src, dst_ref=dst, send_sem=s_sem, recv_sem=r_sem,
            device_id=where, device_id_type=MESH,
        )

    def send(src, dst, s_sem, r_sem, **where):
        copy = remote(src, dst, s_sem, r_sem, **where)
        copy.start()
        pending.append(copy)

    def arrive(dst, s_sem, r_sem, **where):
        remote(dst, dst, s_sem, r_sem, **where).wait_recv()

    barrier = pltpu.get_barrier_semaphore()
    for d in range(1, N):
        pl.semaphore_signal(barrier, inc=1, device_id={"nodes": (me + d) % N}, device_id_type=MESH)
    for d in range(1, M):
        pl.semaphore_signal(barrier, inc=1, device_id={"rep": (rep + d) % M}, device_id_type=MESH)
    pl.semaphore_wait(barrier, N + M - 2)

    def gather_start(buf, l):
        send(buf.at[me], buf.at[me], r_.agp_s.at[l, 0], r_.agp_r.at[l, 0], nodes=partner)
        for d in range(1, NZ):
            to = 2 * ((z + d) % NZ) + par
            send(buf.at[me], buf.at[me], r_.agc_s.at[l, d], r_.agc_r.at[l, d], nodes=to)

    def gather_finish(buf, l):
        for d in range(1, NZ):
            c = 2 * ((z + NZ - d) % NZ) + par
            arrive(buf.at[c], r_.agc_s.at[l, d], r_.agc_r.at[l, d], nodes=c)
            send(buf.at[c], buf.at[c], r_.agp_s.at[l, d], r_.agp_r.at[l, d], nodes=partner)
        for d in range(NZ):
            c = 2 * ((z + NZ - d) % NZ) + 1 - par
            arrive(buf.at[c], r_.agp_s.at[l, d], r_.agp_r.at[l, d], nodes=partner)

    def sync_start(k, tile):
        r_.st1[k, me] = tile
        for d in range(1, N):
            send(r_.st1.at[k, me], r_.st1.at[k, me], r_.st1_s.at[k, d], r_.st1_r.at[k, d], nodes=(me + d) % N)

    def sync_finish(k, combine):
        for d in range(1, N):
            c = (me + N - d) % N
            arrive(r_.st1.at[k, c], r_.st1_s.at[k, d], r_.st1_r.at[k, d], nodes=c)
        r_.st2[k, rep] = combine(r_.st1[k], float(R))
        for d in range(1, M):
            send(r_.st2.at[k, rep], r_.st2.at[k, rep], r_.st2_s.at[k, d], r_.st2_r.at[k, d], rep=(rep + d) % M)
        for d in range(1, M):
            c = (rep + M - d) % M
            arrive(r_.st2.at[k, c], r_.st2_s.at[k, d], r_.st2_r.at[k, d], rep=c)
        return unpack(combine(r_.st2[k], float(R * N)))

    def reduce_step(g, step):
        gs, a1, gt, a2, out = (
            getattr(r_, f"gs{g}"), getattr(r_, f"a1_{g}"), getattr(r_, f"gt{g}"),
            getattr(r_, f"a2_{g}"), (r_.gout0, r_.gout1, r_.gout2)[g],
        )
        rows = gs.shape[0]
        big, small = rows // M, rows // (M * N)
        mine = pl.ds(pl.multiple_of(rep * big, 16), big)
        sub = pl.ds(pl.multiple_of(me * small, 16), small)
        place = lambda p, n: pl.ds(pl.multiple_of(p * big + n * small, 16), small)
        if step == 0:
            for d in range(1, M):
                to = (rep + d) % M
                send(gs.at[pl.ds(pl.multiple_of(to * big, 16), big)], a1.at[rep],
                     r_.ar_s.at[g, 0, d], r_.ar_r.at[g, 0, d], rep=to)
        if step == 1:
            acc = gs[mine].astype(F32)
            for d in range(1, M):
                c = (rep + M - d) % M
                arrive(a1.at[c], r_.ar_s.at[g, 0, d], r_.ar_r.at[g, 0, d], rep=c)
                acc = acc + a1[c].astype(F32)
            gt[...] = acc.astype(BF16)
            for d in range(1, N):
                to = (me + d) % N
                send(gt.at[pl.ds(pl.multiple_of(to * small, 16), small)], a2.at[me],
                     r_.ar_s.at[g, 1, d], r_.ar_r.at[g, 1, d], nodes=to)
        if step == 2:
            acc = gt[sub].astype(F32)
            for d in range(1, N):
                c = (me + N - d) % N
                arrive(a2.at[c], r_.ar_s.at[g, 1, d], r_.ar_r.at[g, 1, d], nodes=c)
                acc = acc + a2[c].astype(F32)
            out[place(rep, me)] = acc.astype(BF16)
            for d in range(1, N):
                here = out.at[place(rep, me)]
                send(here, here, r_.ar_s.at[g, 2, d], r_.ar_r.at[g, 2, d], nodes=(me + d) % N)
        if step == 3:
            for d in range(1, N):
                c = (me + N - d) % N
                arrive(out.at[place(rep, c)], r_.ar_s.at[g, 2, d], r_.ar_r.at[g, 2, d], nodes=c)
            for d in range(1, M):
                send(out.at[mine], out.at[mine], r_.ar_s.at[g, 3, d], r_.ar_r.at[g, 3, d], rep=(rep + d) % M)
        if step == 4:
            for d in range(1, M):
                c = (rep + M - d) % M
                there = pl.ds(pl.multiple_of(c * big, 16), big)
                arrive(out.at[there], r_.ar_s.at[g, 3, d], r_.ar_r.at[g, 3, d], rep=c)

    lane_head = lax.broadcasted_iota(I32, (R, D), 1) // HEAD_DIM

    r_.xs[0, me] = r_.x_in[...]
    r_.meta[me] = r_.meta_in[...]
    for d in range(1, N):
        send(r_.meta.at[me], r_.meta.at[me], r_.meta_s.at[d], r_.meta_r.at[d], nodes=(me + d) % N)
    gather_start(r_.xs.at[0], 0)

    src_row = r_.edges[0:1, :]
    src_row = jnp.where(src_row < R + 24, src_row, src_row + 8)
    dst_row = r_.edges[1:2, :]
    src_col = jnp.broadcast_to(src_row, (128, E)).T[:, 0:1]
    dst_col = jnp.broadcast_to(dst_row, (128, E)).T[:, 0:1]
    as_mask = lambda cond: cond.astype(F32).astype(BF16)
    r_.T[...] = as_mask(dst_col == lax.broadcasted_iota(I32, (E, R), 1))
    r_.TT[...] = as_mask(dst_row == lax.broadcasted_iota(I32, (R, E), 0))
    r_.S[...] = as_mask(src_col == lax.broadcasted_iota(I32, (E, 256), 1))
    r_.ST[...] = as_mask(src_row == lax.broadcasted_iota(I32, (256, E), 0))
    r_.efT[...] = r_.ef[...].T
    for l in range(L):
        r_.ce[l] = dot(r_.ef[...], r_.we[l])
    r_.xf[0] = r_.x_in[...].astype(F32)

    for d in range(1, N):
        c = (me + N - d) % N
        arrive(r_.meta.at[c], r_.meta_s.at[d], r_.meta_r.at[d], nodes=c)
    id_col = jnp.broadcast_to(r_.meta_in[0:1, 0:R], (128, R)).T[:, 0:1]
    id_row = jnp.concatenate([r_.meta[j][0:1, 0:R] for j in range(N)], 1)
    r_.bias[...] = jnp.where(id_col == id_row, 0.0, NEG)

    def halo_onehot(device, start):
        row = jnp.broadcast_to(r_.meta[device][1:2, 0:128], (128, 128)).T[start : start + 24, 0:1]
        hot = (row == lax.broadcasted_iota(I32, (24, R), 1)).astype(F32)
        return jnp.concatenate([hot, jnp.zeros((8, R), F32)], 0).astype(BF16)

    r_.HP[...] = halo_onehot(prev, 24)
    r_.HN[...] = halo_onehot(nxt, 0)
    r_.A[...] = as_mask(r_.meta_in[1:2, 0:64] == lax.broadcasted_iota(I32, (R, 64), 0))

    def layer_forward(l):
        xs = r_.xs
        xb = xs[l, me]
        x = r_.xf[l]
        kv = dot(xs[l].reshape(G, D), r_.wqkv[l, :, D:])
        r_.kk[l] = kv[:, :D].astype(BF16)
        r_.vv[l] = kv[:, D:].astype(BF16)
        r_.q[l] = dot(xb, r_.wqkv[l, :, :D]).astype(BF16).astype(F32)
        r_.xe[l, 0:R] = xb
        r_.xe[l, R : R + 32] = dot(r_.HP[...], xs[l, prev]).astype(BF16)
        r_.xe[l, R + 32 : R + 64] = dot(r_.HN[...], xs[l, nxt]).astype(BF16)
        xe = r_.xe[l]
        tab_b = dot(xe, r_.wp[l, :, D : 2 * D]).astype(BF16)
        tab_e = dot(xe, r_.wp[l, :, 3 * D :]).astype(BF16)
        pa = dot(xb, r_.wp[l, :, 0:D])
        pd = dot(xb, r_.wp[l, :, 2 * D : 3 * D])
        bs = dot(r_.S[...], tab_b)
        r_.bs[l] = bs.astype(BF16)
        gate = sigmoid(select_rows(r_.T[...], pd) + dot(r_.S[...], tab_e) + r_.ce[l])
        r_.gate[l] = gate
        num = select_rows(r_.TT[...], gate * bs)
        den = select_rows(r_.TT[...], gate)
        r_.num[l] = num
        r_.den[l] = den
        msg = pa + num / (den + GATE_EPS)
        r_.z0[l] = msg
        mean0 = col_sum(msg) / R
        sq0 = col_sum((msg - mean0) * (msg - mean0))
        r_.oraw[l] = jnp.zeros((R, D), F32)
        r_.inv[l] = jnp.zeros((R, D), F32)

        def head(h, carry):
            here = lane_head == h
            qm = jnp.where(here, r_.q[l], 0.0).astype(BF16)
            s = dot_nt(qm, r_.kk[l]) + r_.bias[...]
            top = jnp.max(s, 1, keepdims=True)
            e = jnp.exp2((s - top) * (scale * math.log2(math.e)))
            inv = 1.0 / jnp.sum(e, 1, keepdims=True)
            e = e.astype(BF16)
            r_.pst[l, pl.ds(pl.multiple_of(h * R, 64), R)] = e
            o = dot(e, r_.vv[l])
            r_.oraw[l] = jnp.where(here, o * inv, r_.oraw[l])
            r_.inv[l] = jnp.where(here, jnp.broadcast_to(inv, (R, D)), r_.inv[l])
            return carry

        lax.fori_loop(0, HEADS, head, 0)
        ob = r_.oraw[l].astype(BF16)
        r_.ob[l] = ob
        t1 = x + dot(ob, r_.wo[l])
        r_.z1[l] = t1
        mean1 = col_sum(t1) / R
        sq1 = col_sum((t1 - mean1) * (t1 - mean1))
        sync_start(2 * l, pack(mean0, mean1, sq0, sq1))

    def layer_forward_rest(l):
        mean0, mean1, sq0, sq1 = sync_finish(2 * l, combine_pair)
        inv0 = lax.rsqrt(sq0 / total + NORM_EPS)
        inv1 = lax.rsqrt(sq1 / total + NORM_EPS)
        r_.iv[l, 0:1] = inv0
        r_.iv[l, 1:2] = inv1
        z0 = (r_.z0[l] - mean0) * inv0
        z1 = (r_.z1[l] - mean1) * inv1
        r_.z0[l] = z0
        r_.z1[l] = z1
        n0 = z0 * r_.gain[l, 0:1] + r_.shift[l, 0:1]
        mix = r_.xf[l] + n0 * sigmoid(n0) + z1 * r_.gain[l, 1:2] + r_.shift[l, 1:2]
        mb = mix.astype(BF16)
        r_.mb[l] = mb
        u = dot(mb, r_.wu[l])
        r_.u[l] = u
        g = (u * sigmoid(u)).astype(BF16)
        r_.g[l] = g
        return mix + dot(g, r_.wd[l])

    gather_finish(r_.xs.at[0], 0)
    zero_row = jnp.zeros((1, D), F32)
    for l in range(L):
        layer_forward(l)
        y = layer_forward_rest(l)
        r_.z2[l] = y
        mean = col_sum(y) / R
        cent = y - mean
        sq = col_sum(cent * cent)
        gain, shift = r_.gain[l, 2:3], r_.shift[l, 2:3]
        k = 2 * l + 1
        if l < L - 1:
            r_.yc[me] = cent.astype(BF16)
            sync_start(k, pack(mean, zero_row, sq, zero_row))
            gather_start(r_.yc, l + 1)
            tot_mean, _, tot_sq, _ = sync_finish(k, combine_last)
            inv2 = lax.rsqrt(tot_sq / total + NORM_EPS)
            r_.iv[l, 2:3] = inv2
            z2 = (r_.z2[l] - tot_mean) * inv2
            r_.z2[l] = z2
            r_.xf[l + 1] = z2 * gain + shift
            gather_finish(r_.yc, l + 1)
            factor = inv2 * gain
            for j in range(N):
                tile = r_.st1[k, j]
                mean_j = jnp.concatenate([tile[0:1], tile[1:2]], 1)
                moved = (r_.yc[j].astype(F32) + (mean_j - tot_mean)) * factor + shift
                r_.xs[l + 1, j] = moved.astype(BF16)
            r_.xs[l + 1, me] = r_.xf[l + 1].astype(BF16)
        else:
            dy = r_.cot[...].astype(F32)
            sync_start(k, pack(mean, col_sum(dy), sq, col_sum(dy * cent)))
            tot_mean, dy_sum, tot_sq, dy_cent = sync_finish(k, combine_last)
            inv2 = lax.rsqrt(tot_sq / total + NORM_EPS)
            r_.iv[l, 2:3] = inv2
            z2 = (r_.z2[l] - tot_mean) * inv2
            r_.z2[l] = z2
            r_.out_act[...] = z2 * gain + shift
            sums = (dy_sum, dy_cent * inv2)

    def layer_backward(l, dy, sums, mid):
        s2, g2 = sums
        r_.gshift[l, 2:3] = s2
        r_.ggain[l, 2:3] = g2
        d3 = r_.gain[l, 2:3] * r_.iv[l, 2:3] * (dy - s2 / total - r_.z2[l] * (g2 / total))
        db = d3.astype(BF16)
        base = 0 if l == L - 1 else 1280
        gd = dot_tn(r_.g[l], db).astype(BF16)
        r_.gs1[base + 768 : base + 1280] = gd
        dub = (dot_nt(db, r_.wd[l]) * silu_slope(r_.u[l])).astype(BF16)
        dmix = d3 + dot_nt(dub, r_.wu[l])
        r_.dmix[...] = dmix
        n0 = r_.z0[l] * r_.gain[l, 0:1] + r_.shift[l, 0:1]
        gy0 = dmix * silu_slope(n0)
        sync_start(k_back[l], pack(col_sum(dmix), col_sum(dmix * r_.z1[l]), col_sum(gy0), col_sum(gy0 * r_.z0[l])))
        gu = dot_tn(r_.mb[l], dub).astype(BF16)
        r_.gs1[base + 256 : base + 512] = gu[:, 0:D]
        r_.gs1[base + 512 : base + 768] = gu[:, D:]
        q = r_.q[l]
        for h in range(HEADS):
            r_.qm[h * R : (h + 1) * R] = jnp.where(lane_head == h, q, 0.0).astype(BF16)
        r_.qmT[...] = r_.qm[...].T
        s1, g1, s0, g0 = sync_finish(k_back[l], combine_sum)
        r_.gshift[l, 1:2] = s1
        r_.ggain[l, 1:2] = g1
        r_.gshift[l, 0:1] = s0
        r_.ggain[l, 0:1] = g0
        dmix = r_.dmix[...]
        d2 = r_.gain[l, 1:2] * r_.iv[l, 1:2] * (dmix - s1 / total - r_.z1[l] * (g1 / total))
        dab = d2.astype(BF16)
        r_.dxo[...] = dmix + d2
        gs = r_.gs0 if l == L - 1 else r_.gs2
        r_.gs1[base : base + 256] = dot_tn(r_.ob[l], dab).astype(BF16)
        mid(0)
        dob = dot_nt(dab, r_.wo[l]).astype(BF16).astype(F32)
        dos = dob * r_.inv[l]
        prod = dos * r_.oraw[l]
        for h in range(HEADS):
            here = lane_head == h
            r_.dom[h * R : (h + 1) * R] = jnp.where(here, dos, 0.0).astype(BF16)
            r_.delta[h * R : (h + 1) * R] = jnp.sum(jnp.where(here, prod, 0.0), 1, keepdims=True)
        r_.domT[...] = r_.dom[...].T
        r_.gkv[...] = jnp.zeros((2 * D, D), F32)
        W2 = 2 * R

        def block_of(i):
            return (z + 1 + i) % NZ

        def pass_on(i):
            zb = block_of(i)
            arrive(r_.rs1.at[l, zb], r_.rsp_s.at[l, i], r_.rsp_r.at[l, i], nodes=partner)
            both = r_.dxs[l, zb, par].astype(F32) + r_.rs1[l, zb].astype(F32)
            r_.cs[l, zb] = both.astype(BF16)
            remote(r_.cs.at[l, zb], r_.rs2.at[l, z], r_.rsc_s.at[l, i], r_.rsc_r.at[l, i],
                   nodes=2 * zb + par).start()

        def block(i, carry):
            zb = block_of(i)
            cols = pl.ds(pl.multiple_of(zb * W2, 128), W2)
            for h in range(HEADS):
                rows = slice(h * R, (h + 1) * R)
                dp = dot_nt(r_.dom[rows], r_.vv[l, cols])
                ds = r_.pst[l, rows, cols].astype(F32) * (dp - r_.delta[rows])
                r_.dss[rows, cols] = ds.astype(BF16)
            dk = (dot(r_.qmT[...], r_.dss[:, cols]) * scale).astype(BF16)
            dv = dot(r_.domT[...], r_.pst[l, :, cols]).astype(BF16)
            dkv = jnp.concatenate([dk, dv], 0)
            dx = dot(r_.wqkv[l, :, D:], dkv).T
            r_.dxs[l, zb] = dx.astype(BF16).reshape(2, R, D)
            remote(r_.dxs.at[l, zb, 1 - par], r_.rs1.at[l, zb], r_.rsp_s.at[l, i], r_.rsp_r.at[l, i],
                   nodes=partner).start()
            r_.gkv[...] += dot(dkv, r_.xs[l, pl.ds(2 * zb, 2)].reshape(W2, D))

            @pl.when(i > 0)
            def _():
                pass_on(i - 1)

            return carry

        lax.fori_loop(0, NZ, block, 0)
        gkv = r_.gkv[...].T.astype(BF16)
        gs[256:512] = gkv[:, 0:D]
        gs[512:768] = gkv[:, D:]
        mid(1)
        inv_den = 1.0 / (r_.den[l] + GATE_EPS)
        n0 = r_.z0[l] * r_.gain[l, 0:1] + r_.shift[l, 0:1]
        gy0 = r_.dmix[...] * silu_slope(n0)
        dm = r_.gain[l, 0:1] * r_.iv[l, 0:1] * (gy0 - s0 / total - r_.z0[l] * (g0 / total))
        dnum = dm * inv_den
        dden = -dnum * r_.num[l] * inv_den
        dnum_e = select_rows(r_.T[...], dnum)
        dden_e = select_rows(r_.T[...], dden)
        gate = r_.gate[l]
        dgp = (dnum_e * r_.bs[l].astype(F32) + dden_e) * gate * (1.0 - gate)
        dce = dgp.astype(BF16)
        gs[1792:2048] = dot(r_.efT[...], dce).astype(BF16)
        dpb = select_rows(r_.ST[...], dnum_e * gate).astype(BF16)
        dpe = select_rows(r_.ST[...], dgp).astype(BF16)
        dpd = select_rows(r_.TT[...], dgp).astype(BF16)
        dmb = dm.astype(BF16)
        dxe = dot_nt(dpb, r_.wp[l, :, D : 2 * D]) + dot_nt(dpe, r_.wp[l, :, 3 * D :])
        r_.hs[l, 0] = dxe[R : R + 32].astype(BF16)
        r_.hs[l, 1] = dxe[R + 32 : R + 64].astype(BF16)
        send(r_.hs.at[l, 0], r_.hr.at[l, 1], r_.hal_s.at[l, 0], r_.hal_r.at[l, 0], nodes=prev)
        send(r_.hs.at[l, 1], r_.hr.at[l, 0], r_.hal_s.at[l, 1], r_.hal_r.at[l, 1], nodes=nxt)
        r_.dxo[...] += (
            dxe[0:R]
            + dot_nt(dmb, r_.wp[l, :, 0:D])
            + dot_nt(dpd, r_.wp[l, :, 2 * D : 3 * D])
        )
        xeT = r_.xe[l].T
        xbT = r_.xs[l, me].T
        gs[768:1024] = dot(xbT, dmb).astype(BF16)
        gs[1024:1280] = dot(xeT, dpb).astype(BF16)
        gs[1280:1536] = dot(xbT, dpd).astype(BF16)
        gs[1536:1792] = dot(xeT, dpe).astype(BF16)
        dq = jnp.zeros((R, D), F32)
        for h in range(HEADS):
            part = dot(r_.dss[h * R : (h + 1) * R], r_.kk[l])
            dq = jnp.where(lane_head == h, part, dq)
        dqb = (dq * scale).astype(BF16)
        gs[0:256] = dot(xbT, dqb).astype(BF16)
        mid(2)
        dx = r_.dxo[...] + dot_nt(dqb, r_.wqkv[l, :, 0:D])
        arrive(r_.rs1.at[l, z], r_.rsp_s.at[l, NZ - 1], r_.rsp_r.at[l, NZ - 1], nodes=partner)
        dx = dx + r_.dxs[l, z, par].astype(F32) + r_.rs1[l, z].astype(F32)
        for d in range(1, NZ):
            c = (z + NZ - d) % NZ
            arrive(r_.rs2.at[l, c], r_.rsc_s.at[l, d - 1], r_.rsc_r.at[l, d - 1], nodes=2 * c + par)
            dx = dx + r_.rs2[l, c].astype(F32)
        arrive(r_.hr.at[l, 0], r_.hal_s.at[l, 1], r_.hal_r.at[l, 1], nodes=prev)
        arrive(r_.hr.at[l, 1], r_.hal_s.at[l, 0], r_.hal_r.at[l, 0], nodes=nxt)
        back = jnp.concatenate(
            [r_.hr[l, 0].astype(F32)[0:24], r_.hr[l, 1].astype(F32)[0:24], jnp.zeros((16, D), F32)], 0
        )
        dx = dx + dot(r_.A[...], back.astype(BF16))
        for i in range(NZ):
            remote(r_.dxs.at[l, 0, 0], r_.rs1.at[l, 0], r_.rsp_s.at[l, i], r_.rsp_r.at[l, i], nodes=partner).wait_send()
        for i in range(NZ - 1):
            remote(r_.cs.at[l, 0], r_.rs2.at[l, 0], r_.rsc_s.at[l, i], r_.rsc_r.at[l, i], nodes=partner).wait_send()
        return dx

    k_back = {1: 4, 0: 6}
    dx = layer_backward(1, r_.cot[...].astype(F32), sums, lambda stage: reduce_step(0, 0) if stage == 2 else None)
    r_.grad_in[...] = dx
    sync_start(5, pack(col_sum(dx), col_sum(dx * r_.z2[0]), zero_row, zero_row))
    s2, g2, _, _ = sync_finish(5, combine_sum)

    def mid0(stage):
        if stage == 0:
            reduce_step(1, 0)
            reduce_step(0, 1)
        if stage == 1:
            reduce_step(0, 2)
            reduce_step(1, 1)
        if stage == 2:
            reduce_step(2, 0)
            reduce_step(0, 3)
            reduce_step(1, 2)

    dx = layer_backward(0, r_.grad_in[...], (s2, g2), mid0)
    r_.grad_in[...] = dx
    reduce_step(2, 1)
    reduce_step(1, 3)
    reduce_step(2, 2)
    reduce_step(0, 4)
    reduce_step(2, 3)
    reduce_step(1, 4)
    reduce_step(2, 4)
    for copy in pending:
        copy.wait_send()


def unpack_kernel(late1, early, late0, proj, edge, qkv, out, up, down):
    for l, late in ((1, late1), (0, late0)):
        base = 0 if l == 1 else 1280
        for c in range(3):
            qkv[l, :, 256 * c : 256 * c + 256] = late[256 * c : 256 * c + 256].astype(F32)
        for c in range(4):
            proj[l, :, 256 * c : 256 * c + 256] = late[768 + 256 * c : 1024 + 256 * c].astype(F32)
        edge[l] = late[1792:2048].astype(F32)
        out[l] = early[base : base + 256].astype(F32)
        for c in range(2):
            up[l, :, 256 * c : 256 * c + 256] = early[base + 256 * (c + 1) : base + 256 * (c + 2)].astype(F32)
        down[l] = early[base + 768 : base + 1280].astype(F32)


def fused_device(
    N, M, node_input, edge_feat, graph_ids, edge_src, edge_dst, halo_send, w_proj, w_edge, w_qkv,
    w_out, w_up, w_down, norm_gain, norm_shift, cotangent,
):
    R, D = node_input.shape
    E = edge_feat.shape[0]
    L = w_proj.shape[0]
    fill = lambda row, width: jnp.pad(row, (0, width - row.shape[0]), constant_values=-1)
    none = jnp.full((256,), -1, I32)
    meta = jnp.stack([fill(graph_ids, 256), fill(halo_send, 256)] + [none] * 6)
    edges = jnp.stack([edge_src, edge_dst] + [edge_src] * 6)
    names = scratch_list(N, M, L, R, E)
    vmem = pl.BlockSpec(memory_space=pltpu.VMEM)
    shape = jax.ShapeDtypeStruct
    outs = pl.pallas_call(
        functools.partial(kernel, N, M, L, tuple(names)),
        out_shape=[
            shape((R, D), F32), shape((R, D), F32),
            shape((2048, D), BF16), shape((2560, D), BF16), shape((2048, D), BF16),
            shape(norm_gain.shape, F32), shape(norm_gain.shape, F32),
        ],
        in_specs=[vmem] * len(IN_NAMES),
        out_specs=[vmem] * len(OUT_NAMES),
        scratch_shapes=list(names.values()),
        compiler_params=pltpu.CompilerParams(
            collective_id=0, has_side_effects=True, vmem_limit_bytes=60 << 20
        ),
        name="layers",
    )(node_input, meta, edges, edge_feat, w_proj, w_edge, w_qkv, w_out, w_up, w_down,
      norm_gain, norm_shift, cotangent)
    out_act, grad_in, late1, early, late0, ggain, gshift = outs
    grads = pl.pallas_call(
        unpack_kernel,
        out_shape=[shape(w.shape, F32) for w in (w_proj, w_edge, w_qkv, w_out, w_up, w_down)],
        in_specs=[vmem] * 3,
        out_specs=[vmem] * 6,
        compiler_params=pltpu.CompilerParams(vmem_limit_bytes=40 << 20),
        name="gradients",
    )(late1, early, late0)
    return (out_act, grad_in, *grads, ggain, gshift)


BLOCK_CAP = 2048


def extended_2(block, sides, width):
    for axis, dim in sides:
        count = lax.axis_size(axis)
        forward = [(i, i + 1) for i in range(count - 1)]
        forward.append((count - 1, 0))
        backward = [(target, source) for source, target in forward]
        low = lax.ppermute(
            lax.slice_in_dim(block, block.shape[dim] - width, None, axis=dim), axis, forward
        )
        high = lax.ppermute(lax.slice_in_dim(block, 0, width, axis=dim), axis, backward)
        block = jnp.concatenate([low, block, high], axis=dim)
    return block


def block_length(total_rows, upper_limit):
    for length in range(min(total_rows, upper_limit), 0, -1):
        if total_rows % length == 0:
            return length
    return 1


def outer_product(left, right):
    return lax.dot_general(
        left, right, (((0,), (0,)), ((), ())), preferred_element_type=jnp.float32
    )


def times_transposed(left, weight):
    return lax.dot_general(
        left, weight, (((1,), (1,)), ((), ())), preferred_element_type=jnp.float32
    )


def forward_product(left, weight):
    return jnp.dot(left, weight, preferred_element_type=jnp.float32)


def silu_slope_plain(inputs):
    logistic = jax.nn.sigmoid(inputs)
    return logistic * (1.0 + inputs * (1.0 - logistic))


def normalize(inputs, gain_row, shift_row, node_total):
    batch_mean = lax.psum(jnp.sum(inputs, 0), ("nodes", "rep")) / node_total
    centred = inputs - batch_mean
    batch_var = lax.psum(jnp.sum(centred * centred, 0), ("nodes", "rep")) / node_total
    inv_std = lax.rsqrt(batch_var + NORM_EPS)
    standard = (inputs - batch_mean) * inv_std
    return (standard * gain_row + shift_row, standard, inv_std)


def normalize_back(grad_out, standard, inv_std, gain_row, node_total):
    shift_grad, gain_grad = lax.psum(
        (jnp.sum(grad_out, 0), jnp.sum(grad_out * standard, 0)), ("nodes", "rep")
    )
    grad_in = (
        gain_row
        * inv_std
        * (grad_out - shift_grad / node_total - standard * gain_grad / node_total)
    )
    return (grad_in, gain_grad, shift_grad)


def exchange_sources(outgoing):
    halo_rows = outgoing.shape[0] // 2
    grown = extended_2(outgoing, (("nodes", 0),), halo_rows)
    return jnp.concatenate([grown[:halo_rows], grown[3 * halo_rows :]], 0)


def return_sources(incoming_grad):
    halo_rows = incoming_grad.shape[0] // 2
    grown = extended_2(incoming_grad.astype(jnp.bfloat16), (("nodes", 0),), halo_rows).astype(
        incoming_grad.dtype
    )
    return jnp.concatenate([grown[:halo_rows], grown[3 * halo_rows :]], 0)


def attend_forward(query_rows, key_rows, value_rows, local_graphs, group_graphs):
    row_count = query_rows.shape[0]
    score_scale = HEAD_DIM ** (-0.5)
    queries = query_rows.reshape(row_count, HEADS, HEAD_DIM)

    def add_piece(carried, kv_piece, first_row):
        key_piece, value_piece = kv_piece
        piece_rows = key_piece.shape[0]
        block_len = block_length(piece_rows, BLOCK_CAP)

        def add_block(block_state, block_index):
            row_max, row_sum, accumulated = block_state
            block_start = block_index * block_len
            key_block = lax.dynamic_slice_in_dim(key_piece, block_start, block_len, 0).reshape(
                block_len, HEADS, HEAD_DIM
            )
            value_block = lax.dynamic_slice_in_dim(value_piece, block_start, block_len, 0).reshape(
                block_len, HEADS, HEAD_DIM
            )
            key_graphs = lax.dynamic_slice_in_dim(
                group_graphs, first_row + block_start, block_len, 0
            )
            same_graph = (local_graphs[:, None] == key_graphs[None, :])[None]
            scores = (
                jnp.einsum("qhd,khd->hqk", queries, key_block, preferred_element_type=jnp.float32)
                * score_scale
            )
            scores = jnp.where(same_graph, scores, NEG)
            new_max = jnp.maximum(row_max, jnp.max(scores, 2))
            weights = jnp.where(same_graph, jnp.exp(scores - new_max[:, :, None]), 0.0)
            factor = jnp.exp(row_max - new_max)
            row_sum = row_sum * factor + jnp.sum(weights, 2)
            contrib = jnp.einsum(
                "hqk,khd->qhd",
                weights.astype(jnp.bfloat16),
                value_block,
                preferred_element_type=jnp.float32,
            )
            accumulated = accumulated * jnp.transpose(factor)[:, :, None] + contrib
            return ((new_max, row_sum, accumulated), None)

        carried, _ = lax.scan(add_block, carried, jnp.arange(piece_rows // block_len))
        return carried

    start_state = (
        jnp.full((HEADS, row_count), NEG, jnp.float32),
        jnp.zeros((HEADS, row_count), jnp.float32),
        jnp.zeros((row_count, HEADS, HEAD_DIM), jnp.float32),
    )
    row_max, row_sum, accumulated = add_piece(
        start_state,
        (
            lax.all_gather(key_rows, "nodes", axis=0, tiled=True),
            lax.all_gather(value_rows, "nodes", axis=0, tiled=True),
        ),
        jnp.int32(0),
    )
    attn_raw = accumulated / jnp.transpose(row_sum)[:, :, None]
    log_sum = row_max + jnp.log(row_sum)
    return (attn_raw, log_sum)


def attend_backward(
    query_rows, key_rows, value_rows, grad_low, attn_raw, log_sum, local_graphs, group_graphs
):
    row_count = query_rows.shape[0]
    model_width = HEADS * HEAD_DIM
    score_scale = HEAD_DIM ** (-0.5)
    queries = query_rows.reshape(row_count, HEADS, HEAD_DIM)
    grad_heads = grad_low.reshape(row_count, HEADS, HEAD_DIM)
    row_delta = jnp.einsum("qhd,qhd->hq", grad_heads.astype(jnp.float32), attn_raw)

    def score_block(key_block, value_block, key_graphs):
        same_graph = (local_graphs[:, None] == key_graphs[None, :])[None]
        scores = (
            jnp.einsum("qhd,khd->hqk", queries, key_block, preferred_element_type=jnp.float32)
            * score_scale
        )
        attn_weights = jnp.exp(jnp.where(same_graph, scores - log_sum[:, :, None], NEG))
        grad_weights = jnp.einsum(
            "qhd,khd->hqk", grad_heads, value_block, preferred_element_type=jnp.float32
        )
        grad_scores = (attn_weights * (grad_weights - row_delta[:, :, None])).astype(jnp.bfloat16)
        return (attn_weights, grad_scores)

    def key_terms(attn_weights, grad_scores, block_len):
        grad_keys = (
            jnp.einsum("hqk,qhd->khd", grad_scores, queries, preferred_element_type=jnp.float32)
            * score_scale
        )
        grad_values = jnp.einsum(
            "hqk,qhd->khd",
            attn_weights.astype(jnp.bfloat16),
            grad_heads,
            preferred_element_type=jnp.float32,
        )
        return jnp.concatenate(
            [
                grad_keys.reshape(block_len, model_width),
                grad_values.reshape(block_len, model_width),
            ],
            1,
        )

    def query_term(grad_scores, key_block):
        return (
            jnp.einsum("hqk,khd->qhd", grad_scores, key_block, preferred_element_type=jnp.float32)
            * score_scale
        )

    group_rows = group_graphs.shape[0]

    def add_piece(carried, kv_piece, first_row):
        key_piece, value_piece = kv_piece
        piece_rows = key_piece.shape[0]
        block_len = block_length(piece_rows, BLOCK_CAP)

        def add_block(block_state, block_index):
            grad_query, buffer = block_state
            block_start = block_index * block_len
            key_block = lax.dynamic_slice_in_dim(key_piece, block_start, block_len, 0).reshape(
                block_len, HEADS, HEAD_DIM
            )
            value_block = lax.dynamic_slice_in_dim(value_piece, block_start, block_len, 0).reshape(
                block_len, HEADS, HEAD_DIM
            )
            place = first_row + block_start
            key_graphs = lax.dynamic_slice_in_dim(group_graphs, place, block_len, 0)
            attn_weights, grad_scores = score_block(key_block, value_block, key_graphs)
            grad_query = grad_query + query_term(grad_scores, key_block)
            block_terms = key_terms(attn_weights, grad_scores, block_len)
            current = lax.dynamic_slice_in_dim(buffer, place, block_len, 0)
            buffer = lax.dynamic_update_slice_in_dim(buffer, current + block_terms, place, 0)
            return ((grad_query, buffer), None)

        carried, _ = lax.scan(add_block, carried, jnp.arange(piece_rows // block_len))
        return carried

    start_state = (
        jnp.zeros((row_count, HEADS, HEAD_DIM), jnp.float32),
        jnp.zeros((group_rows, 2 * model_width), jnp.float32),
    )
    grad_query, buffer = add_piece(
        start_state,
        (
            lax.all_gather(key_rows, "nodes", axis=0, tiled=True),
            lax.all_gather(value_rows, "nodes", axis=0, tiled=True),
        ),
        jnp.int32(0),
    )
    grad_kv = lax.psum_scatter(buffer, "nodes", scatter_dimension=0, tiled=True)
    return (
        grad_query.reshape(row_count, model_width),
        grad_kv[:, :model_width],
        grad_kv[:, model_width:],
    )


def layer_forward(
    hidden, params, edge_feat, edge_src, edge_dst, halo_send, local_graphs, group_graphs, node_total
):
    w_proj, w_edge, w_qkv, w_out, w_up, w_down, norm_gains, norm_shifts = params
    row_count, model_width = hidden.shape
    hidden_low = hidden.astype(jnp.bfloat16)
    projected = forward_product(hidden_low, w_proj)
    self_term = projected[:, :model_width]
    dest_term = projected[:, 2 * model_width : 3 * model_width]
    source_rows = jnp.concatenate(
        [projected[:, model_width : 2 * model_width], projected[:, 3 * model_width :]], 1
    ).astype(jnp.bfloat16)
    incoming = exchange_sources(source_rows[halo_send])
    extended = jnp.concatenate([source_rows, incoming], 0)
    edge_rows = extended[edge_src].astype(jnp.float32)
    source_b = edge_rows[:, :model_width]
    source_e = edge_rows[:, model_width:]
    edge_proj = forward_product(edge_feat, w_edge)
    gating = jax.nn.sigmoid(dest_term[edge_dst] + source_e + edge_proj)
    numerator = jax.ops.segment_sum(gating * source_b, edge_dst, row_count)
    denominator = jax.ops.segment_sum(gating, edge_dst, row_count)
    message = self_term + numerator / (denominator + GATE_EPS)
    normed_one, standard_one, inv_one = normalize(
        message, norm_gains[0], norm_shifts[0], node_total
    )
    local_out = hidden + jax.nn.silu(normed_one)
    qkv_low = forward_product(hidden_low, w_qkv).astype(jnp.bfloat16)
    query_rows = qkv_low[:, :model_width]
    key_rows = qkv_low[:, model_width : 2 * model_width]
    value_rows = qkv_low[:, 2 * model_width :]
    attn_raw, log_sum = attend_forward(query_rows, key_rows, value_rows, local_graphs, group_graphs)
    attn_low = attn_raw.reshape(row_count, model_width).astype(jnp.bfloat16)
    attn_proj = forward_product(attn_low, w_out)
    normed_two, standard_two, inv_two = normalize(
        hidden + attn_proj, norm_gains[1], norm_shifts[1], node_total
    )
    mixed = local_out + normed_two
    mixed_low = mixed.astype(jnp.bfloat16)
    up_proj = forward_product(mixed_low, w_up)
    activated = jax.nn.silu(up_proj).astype(jnp.bfloat16)
    down_proj = forward_product(activated, w_down)
    normed_three, standard_three, inv_three = normalize(
        mixed + down_proj, norm_gains[2], norm_shifts[2], node_total
    )
    saved = (
        hidden_low,
        source_b,
        gating,
        numerator,
        denominator,
        normed_one,
        standard_one,
        inv_one,
        query_rows,
        key_rows,
        value_rows,
        attn_raw,
        log_sum,
        attn_low,
        standard_two,
        inv_two,
        mixed_low,
        up_proj,
        activated,
        standard_three,
        inv_three,
    )
    return (normed_three, saved)


def layer_backward(
    grad_out,
    params,
    saved,
    edge_feat,
    edge_src,
    edge_dst,
    halo_send,
    local_graphs,
    group_graphs,
    node_total,
):
    w_proj, w_edge, w_qkv, w_out, w_up, w_down, norm_gains, norm_shifts = params
    (
        hidden_low,
        source_b,
        gating,
        numerator,
        denominator,
        normed_one,
        standard_one,
        inv_one,
        query_rows,
        key_rows,
        value_rows,
        attn_raw,
        log_sum,
        attn_low,
        standard_two,
        inv_two,
        mixed_low,
        up_proj,
        activated,
        standard_three,
        inv_three,
    ) = saved
    row_count, model_width = grad_out.shape
    grad_three, gain_three, shift_three = normalize_back(
        grad_out, standard_three, inv_three, norm_gains[2], node_total
    )
    down_grad = grad_three.astype(jnp.bfloat16)
    grad_w_down = outer_product(activated, down_grad)
    up_grad = (times_transposed(down_grad, w_down) * silu_slope_plain(up_proj)).astype(jnp.bfloat16)
    grad_w_up = outer_product(mixed_low, up_grad)
    grad_mixed = grad_three + times_transposed(up_grad, w_up)
    grad_two, gain_two, shift_two = normalize_back(
        grad_mixed, standard_two, inv_two, norm_gains[1], node_total
    )
    out_grad = grad_two.astype(jnp.bfloat16)
    grad_w_out = outer_product(attn_low, out_grad)
    attn_grad = times_transposed(out_grad, w_out).astype(jnp.bfloat16)
    grad_query, grad_key, grad_value = attend_backward(
        query_rows, key_rows, value_rows, attn_grad, attn_raw, log_sum, local_graphs, group_graphs
    )
    qkv_grad = jnp.concatenate([grad_query, grad_key, grad_value], 1).astype(jnp.bfloat16)
    grad_w_qkv = outer_product(hidden_low, qkv_grad)
    grad_message, gain_one, shift_one = normalize_back(
        grad_mixed * silu_slope_plain(normed_one), standard_one, inv_one, norm_gains[0], node_total
    )
    shifted = denominator + GATE_EPS
    grad_numer = grad_message / shifted
    grad_denom = -grad_message * numerator / (shifted * shifted)
    numer_edge = grad_numer[edge_dst]
    grad_gate = numer_edge * source_b + grad_denom[edge_dst]
    grad_pre_edge = grad_gate * gating * (1.0 - gating)
    edge_grad = grad_pre_edge.astype(jnp.bfloat16)
    grad_w_edge = outer_product(edge_feat, edge_grad)
    grad_dest = jax.ops.segment_sum(grad_pre_edge, edge_dst, row_count)
    grad_extended = jax.ops.segment_sum(
        jnp.concatenate([numer_edge * gating, grad_pre_edge], 1),
        edge_src,
        row_count + halo_send.shape[0],
    )
    returned = return_sources(grad_extended[row_count:])
    grad_source = grad_extended[:row_count].at[halo_send].add(returned)
    proj_grad = jnp.concatenate(
        [grad_message, grad_source[:, :model_width], grad_dest, grad_source[:, model_width:]], 1
    ).astype(jnp.bfloat16)
    grad_w_proj = outer_product(hidden_low, proj_grad)
    grad_hidden = (
        grad_mixed
        + grad_two
        + times_transposed(proj_grad, w_proj)
        + times_transposed(qkv_grad, w_qkv)
    )
    weight_grads = (grad_w_proj, grad_w_edge, grad_w_qkv, grad_w_out, grad_w_up, grad_w_down)
    return (
        grad_hidden,
        weight_grads,
        jnp.stack([gain_one, gain_two, gain_three]),
        jnp.stack([shift_one, shift_two, shift_three]),
    )


def per_device(
    node_input,
    edge_feat,
    graph_ids,
    edge_src,
    edge_dst,
    halo_send,
    w_proj,
    w_edge,
    w_qkv,
    w_out,
    w_up,
    w_down,
    norm_gain,
    norm_shift,
    cotangent,
):
    group_graphs = lax.all_gather(graph_ids, "nodes", axis=0, tiled=True)
    node_total = node_input.shape[0] * lax.axis_size("nodes") * lax.axis_size("rep")
    layer_count = w_proj.shape[0]
    layer_params = [
        (
            w_proj[layer_index],
            w_edge[layer_index],
            w_qkv[layer_index],
            w_out[layer_index],
            w_up[layer_index],
            w_down[layer_index],
            norm_gain[layer_index],
            norm_shift[layer_index],
        )
        for layer_index in range(layer_count)
    ]
    hidden = node_input.astype(jnp.float32)
    saved_all = []
    for layer_index in range(layer_count):
        hidden, saved = layer_forward(
            hidden,
            layer_params[layer_index],
            edge_feat,
            edge_src,
            edge_dst,
            halo_send,
            graph_ids,
            group_graphs,
            node_total,
        )
        saved_all.append(saved)
    grad_hidden = cotangent.astype(jnp.float32)
    weight_parts = [None] * layer_count
    gain_parts = [None] * layer_count
    shift_parts = [None] * layer_count
    for layer_index in range(layer_count - 1, -1, -1):
        (
            grad_hidden,
            weight_parts[layer_index],
            gain_parts[layer_index],
            shift_parts[layer_index],
        ) = layer_backward(
            grad_hidden,
            layer_params[layer_index],
            saved_all[layer_index],
            edge_feat,
            edge_src,
            edge_dst,
            halo_send,
            graph_ids,
            group_graphs,
            node_total,
        )
    proj_local = jnp.stack([weight_parts[layer_index][0] for layer_index in range(layer_count)])
    edge_local = jnp.stack([weight_parts[layer_index][1] for layer_index in range(layer_count)])
    qkv_local = jnp.stack([weight_parts[layer_index][2] for layer_index in range(layer_count)])
    out_local = jnp.stack([weight_parts[layer_index][3] for layer_index in range(layer_count)])
    up_local = jnp.stack([weight_parts[layer_index][4] for layer_index in range(layer_count)])
    down_local = jnp.stack([weight_parts[layer_index][5] for layer_index in range(layer_count)])
    grad_proj, grad_edge, grad_qkv, grad_out, grad_up, grad_down = lax.psum(
        (proj_local, edge_local, qkv_local, out_local, up_local, down_local), ("nodes", "rep")
    )
    return (
        hidden,
        grad_hidden,
        grad_proj,
        grad_edge,
        grad_qkv,
        grad_out,
        grad_up,
        grad_down,
        jnp.stack(gain_parts),
        jnp.stack(shift_parts),
    )


def solution(mesh):
    in_specs = (
        P(("rep", "nodes"), None),
        P(("rep", "nodes"), None),
        P(("rep", "nodes")),
        P(("rep", "nodes")),
        P(("rep", "nodes")),
        P(("rep", "nodes")),
        P(),
        P(),
        P(),
        P(),
        P(),
        P(),
        P(),
        P(),
        P(("rep", "nodes"), None),
    )
    out_specs = (
        P(("rep", "nodes"), None),
        P(("rep", "nodes"), None),
        P(),
        P(),
        P(),
        P(),
        P(),
        P(),
        P(),
        P(),
    )
    N, M = mesh.shape["nodes"], mesh.shape["rep"]
    fused = N % 2 == 0 and N <= 8 and 2048 % (16 * N * M) == 0 and 2560 % (16 * N * M) == 0
    return jax.shard_map(
        functools.partial(fused_device, N, M) if fused else per_device,
        mesh=mesh, in_specs=in_specs, out_specs=out_specs, check_vma=False,
    )
```

```python
import functools
import math

import jax
import jax.numpy as jnp
from jax import lax
from jax.experimental import pallas as pl
from jax.experimental.pallas import tpu as pltpu
from jax.sharding import PartitionSpec as P

HEADS = 8
HEAD_DIM = 32
NEG = -1e30
NORM_EPS = 1e-05
GATE_EPS = 1e-06
F32, BF16, I32 = jnp.float32, jnp.bfloat16, jnp.int32
MESH = pl.DeviceIdType.MESH
SYNCS = 7
GROUPS = ((2048, "rep"), (2560, "rep"), (1024, "rep"), (512, "rep"), (512, "nodes"))


def dot(left, right):
    return lax.dot_general(
        left, right, (((1,), (0,)), ((), ())), preferred_element_type=F32
    )


def dot_nt(left, right):
    return lax.dot_general(
        left, right, (((1,), (1,)), ((), ())), preferred_element_type=F32
    )


def dot_tn(left, right):
    return lax.dot_general(
        left, right, (((0,), (0,)), ((), ())), preferred_element_type=F32
    )


def split(value):
    high = value.astype(BF16)
    return high, (value - high.astype(F32)).astype(BF16)


def select_rows(onehot, value):
    high, low = split(value)
    return dot(onehot, high) + dot(onehot, low)


def sigmoid(value):
    return 1.0 / (1.0 + jnp.exp(-value))


def silu_slope(value):
    logistic = sigmoid(value)
    return logistic * (1.0 + value * (1.0 - logistic))


def col_sum(value):
    return jnp.sum(value, axis=0, keepdims=True)


def pack(first, second, third, fourth):
    halves = []
    for row in (first, second, third, fourth):
        halves += [row[:, :128], row[:, 128:]]
    return jnp.concatenate(halves, 0)


def unpack(tile):
    return [
        jnp.concatenate([tile[2 * i : 2 * i + 1], tile[2 * i + 1 : 2 * i + 2]], 1)
        for i in range(4)
    ]


def combine_pair(tiles, count):
    mean = jnp.mean(tiles[:, 0:4], 0)
    off = tiles[:, 0:4] - mean
    return jnp.concatenate([mean, jnp.sum(tiles[:, 4:8] + count * off * off, 0)], 0)


def combine_last(tiles, count):
    mean = jnp.mean(tiles[:, 0:2], 0)
    off = tiles[:, 0:2] - mean
    return jnp.concatenate(
        [
            mean,
            jnp.sum(tiles[:, 2:4], 0),
            jnp.sum(tiles[:, 4:6] + count * off * off, 0),
            jnp.sum(tiles[:, 6:8] + off * tiles[:, 2:4], 0),
        ],
        0,
    )


def combine_sum(tiles, count):
    return jnp.sum(tiles, 0)


class Refs:
    pass


def scratch_list(N, M, L, R, E):
    NZ, G, HR = N // 2, N * R, HEADS * R
    D, FF = 256, 512
    dma = lambda *shape: pltpu.SemaphoreType.DMA(shape)
    vm = lambda dtype, *shape: pltpu.VMEM(shape, dtype)
    names = dict(
        xs=vm(BF16, L, N, R, D),
        yc=vm(BF16, N, R, D),
        meta=vm(I32, N, 8, 256),
        ef=vm(BF16, E, D),
        cot=vm(BF16, R, D),
        wp=vm(BF16, L, D, 4 * D),
        we=vm(BF16, L, D, D),
        wqkv=vm(BF16, L, D, 3 * D),
        wo=vm(BF16, L, D, D),
        wu=vm(BF16, L, D, FF),
        wd=vm(BF16, L, FF, D),
        oact=vm(F32, R, D),
        gin=vm(F32, R, D),
        dce=vm(BF16, E, D),
        dproj=vm(BF16, 4, 256, D),
        xeT=vm(BF16, L, D, 256),
        st1=vm(F32, SYNCS, N, 8, 128),
        st2=vm(F32, SYNCS, M, 8, 128),
        T=vm(BF16, E, R),
        TT=vm(BF16, R, E),
        S=vm(BF16, E, 256),
        ST=vm(BF16, 256, E),
        efT=vm(BF16, D, E),
        HP=vm(BF16, 32, R),
        HN=vm(BF16, 32, R),
        A=vm(BF16, R, 64),
        bias=vm(F32, R, G),
        ce=vm(F32, L, E, D),
        xf=vm(F32, L, R, D),
        xe=vm(BF16, L, 256, D),
        gate=vm(F32, L, E, D),
        bs=vm(BF16, L, E, D),
        num=vm(F32, L, R, D),
        den=vm(F32, L, R, D),
        z0=vm(F32, L, R, D),
        z1=vm(F32, L, R, D),
        z2=vm(F32, L, R, D),
        q=vm(F32, L, R, D),
        kk=vm(BF16, L, G, D),
        vv=vm(BF16, L, G, D),
        pst=vm(BF16, L, HR, G),
        oraw=vm(F32, L, R, D),
        inv=vm(F32, L, R, D),
        ob=vm(BF16, L, R, D),
        mb=vm(BF16, L, R, D),
        u=vm(F32, L, R, FF),
        g=vm(BF16, L, R, FF),
        iv=vm(F32, L, 8, D),
        dmix=vm(F32, R, D),
        dxo=vm(F32, R, D),
        qm=vm(BF16, HR, D),
        qmT=vm(BF16, D, HR),
        dom=vm(BF16, HR, D),
        domT=vm(BF16, D, HR),
        delta=vm(F32, HR, 1),
        dss=vm(BF16, HR, G),
        gkv=vm(F32, 2 * D, D),
        dxs=vm(BF16, L, NZ, 2, R, D),
        rs1=vm(BF16, L, NZ, R, D),
        cs=vm(BF16, L, NZ, R, D),
        rs2=vm(BF16, L, NZ, R, D),
        hs=vm(BF16, L, 2, 32, D),
        hr=vm(BF16, L, 2, 32, D),
    )
    for g, (rows, first) in enumerate(GROUPS):
        a, b = (N, M) if first == "nodes" else (M, N)
        names[f"gs{g}"] = vm(BF16, rows, D)
        names[f"a1_{g}"] = vm(BF16, a, rows // a, D)
        names[f"gt{g}"] = vm(BF16, rows // a, D)
        names[f"a2_{g}"] = vm(BF16, b, rows // (M * N), D)
        names[f"gf{g}"] = vm(BF16, rows // (M * N), D)
    names.update(
        load=dma(10),
        store=dma(2),
        meta_s=dma(1),
        meta_r=dma(1),
        st1_s=dma(SYNCS),
        st1_r=dma(SYNCS),
        st2_s=dma(SYNCS),
        st2_r=dma(SYNCS),
        agc_s=dma(L, NZ),
        agc_r=dma(L, NZ),
        agp_s=dma(L, NZ),
        agp_r=dma(L, NZ),
        rsp_s=dma(L, NZ),
        rsp_r=dma(L, NZ),
        rsc_s=dma(L, NZ),
        rsc_r=dma(L, NZ),
        hal_s=dma(L, 2),
        hal_r=dma(L, 2),
        ar_s=dma(len(GROUPS), 4),
        ar_r=dma(len(GROUPS), 4),
        ar_l=dma(len(GROUPS)),
    )
    return names


IN_NAMES = (
    "x_in", "ids", "edge_src", "edge_dst", "halo", "ef_h", "wp_h", "we_h", "wqkv_h", "wo_h", "wu_h", "wd_h",
    "gain", "shift", "cot_h",
)
OUT_NAMES = ("out_act", "grad_in", "gout0", "gout1", "gout2", "gout3", "gout4", "ggain", "gshift")


def kernel(N, M, L, names, *args):
    r_ = Refs()
    for name, ref in zip(IN_NAMES + OUT_NAMES + tuple(names), args, strict=True):
        setattr(r_, name, ref)
    R, D = r_.x_in.shape
    E = r_.ef.shape[0]
    NZ, G, HR = N // 2, N * R, HEADS * R
    total = float(N * M * R)
    scale = HEAD_DIM ** -0.5
    me = lax.axis_index("nodes")
    rep = lax.axis_index("rep")
    z = me // 2
    par = me % 2
    partner = 2 * z + (1 - par)
    prev = (me + N - 1) % N
    nxt = (me + 1) % N
    drains = []

    def remote(src, dst, s_sem, r_sem, **where):
        return pltpu.make_async_remote_copy(
            src_ref=src, dst_ref=dst, send_sem=s_sem, recv_sem=r_sem,
            device_id=where, device_id_type=MESH,
        )

    def send(src, dst, s_sem, r_sem, **where):
        remote(src, dst, s_sem, r_sem, **where).start()

    def arrive(dst, r_sem):
        remote(dst, dst, r_sem, r_sem, nodes=partner).wait_recv()

    def sent(src, s_sem):
        drains.append((src, s_sem))

    loads = [
        pltpu.make_async_copy(getattr(r_, f"{name}_h"), getattr(r_, name), r_.load.at[i])
        for i, name in enumerate(("ef", "we", "wqkv", "wp", "wo", "wu", "wd", "cot"))
    ]
    own_rows = pltpu.make_async_copy(r_.x_in, r_.xs.at[0, me], r_.load.at[8])
    own_rows.start()
    for load in loads:
        load.start()

    barrier = pltpu.get_barrier_semaphore()
    for d in range(1, N):
        pl.semaphore_signal(barrier, inc=1, device_id={"nodes": (me + d) % N}, device_id_type=MESH)
    for d in range(1, M):
        pl.semaphore_signal(barrier, inc=1, device_id={"rep": (rep + d) % M}, device_id_type=MESH)
    pl.semaphore_wait(barrier, N + M - 2)

    def gather_start(buf, l):
        send(buf.at[me], buf.at[me], r_.agp_s.at[l, 0], r_.agp_r.at[l, 0], nodes=partner)
        sent(buf.at[me], r_.agp_s.at[l, 0])
        for d in range(1, NZ):
            to = 2 * ((z + d) % NZ) + par
            send(buf.at[me], buf.at[me], r_.agc_s.at[l, d], r_.agc_r.at[l, d], nodes=to)
            sent(buf.at[me], r_.agc_s.at[l, d])

    def gather_finish(buf, l):
        for d in range(1, NZ):
            c = 2 * ((z + NZ - d) % NZ) + par
            arrive(buf.at[c], r_.agc_r.at[l, d])
            send(buf.at[c], buf.at[c], r_.agp_s.at[l, d], r_.agp_r.at[l, d], nodes=partner)
            sent(buf.at[c], r_.agp_s.at[l, d])
        for d in range(NZ):
            c = 2 * ((z + NZ - d) % NZ) + 1 - par
            arrive(buf.at[c], r_.agp_r.at[l, d])

    def sync_start(k, tile):
        r_.st1[k, me] = tile
        for d in range(1, N):
            send(r_.st1.at[k, me], r_.st1.at[k, me], r_.st1_s.at[k], r_.st1_r.at[k], nodes=(me + d) % N)
        sent(r_.st1.at[k, 0 : N - 1], r_.st1_s.at[k])

    def sync_finish(k, combine):
        arrive(r_.st1.at[k, 0 : N - 1], r_.st1_r.at[k])
        r_.st2[k, rep] = combine(r_.st1[k], float(R))
        for d in range(1, M):
            send(r_.st2.at[k, rep], r_.st2.at[k, rep], r_.st2_s.at[k], r_.st2_r.at[k], rep=(rep + d) % M)
        sent(r_.st2.at[k, 0 : M - 1], r_.st2_s.at[k])
        arrive(r_.st2.at[k, 0 : M - 1], r_.st2_r.at[k])
        return unpack(combine(r_.st2[k], float(R * N)))

    def reduce_step(g, step):
        gs, a1, gt, a2, gf, out = (
            getattr(r_, f"{name}{g}") for name in ("gs", "a1_", "gt", "a2_", "gf", "gout")
        )
        rows, first = GROUPS[g]
        if first == "rep":
            one, two, n1, n2, i1, i2 = "rep", "nodes", M, N, rep, me
        else:
            one, two, n1, n2, i1, i2 = "nodes", "rep", N, M, me, rep
        big, small = rows // n1, rows // (M * N)
        part = lambda i, size: pl.ds(pl.multiple_of(i * size, 16), size)
        final = pl.ds(pl.multiple_of(i1 * big + i2 * small, 16), small)
        s_sem, r_sem = r_.ar_s.at[g, min(step, 3)], r_.ar_r.at[g, min(step, 3)]
        if step > 0:
            was = r_.ar_r.at[g, step - 1]
        if step == 0:
            for d in range(1, n1):
                to = (i1 + d) % n1
                send(gs.at[part(to, big)], a1.at[i1], s_sem, r_sem, **{one: to})
        if step == 1:
            arrive(a1.at[0 : n1 - 1], was)
            acc = gs[part(i1, big)].astype(F32)
            for d in range(1, n1):
                acc = acc + a1[(i1 + d) % n1].astype(F32)
            gt[...] = acc.astype(BF16)
            for d in range(1, n2):
                to = (i2 + d) % n2
                send(gt.at[part(to, small)], a2.at[i2], s_sem, r_sem, **{two: to})
        if step == 2:
            arrive(a2.at[0 : n2 - 1], was)
            acc = gt[part(i2, small)].astype(F32)
            for d in range(1, n2):
                acc = acc + a2[(i2 + d) % n2].astype(F32)
            gf[...] = acc.astype(BF16)
            pltpu.make_async_copy(gf, out.at[final], r_.ar_l.at[g]).start()
            for d in range(1, n2):
                send(gf, out.at[final], s_sem, r_sem, **{two: (i2 + d) % n2})
        if step == 3:
            pltpu.make_async_copy(gf, out.at[final], r_.ar_l.at[g]).wait()
            arrive(out.at[0 : (n2 - 1) * small], was)
            for d in range(1, n1):
                send(out.at[part(i1, big)], out.at[part(i1, big)], s_sem, r_sem, **{one: (i1 + d) % n1})
        if step == 4:
            arrive(out.at[0 : (n1 - 1) * big], was)

    def reduce_drain(g):
        rows, first = GROUPS[g]
        n1, n2 = (M, N) if first == "rep" else (N, M)
        gs = getattr(r_, f"gs{g}")
        for step, count in enumerate(
            ((n1 - 1) * (rows // n1), (n2 - 1) * (rows // (M * N)), (n2 - 1) * (rows // (M * N)), (n1 - 1) * (rows // n1))
        ):
            sent(gs.at[0:count], r_.ar_s.at[g, step])

    lane_head = lax.broadcasted_iota(I32, (R, D), 1) // HEAD_DIM

    r_.meta[me] = jnp.full((8, 256), -1, I32)
    r_.meta[me, 0:1, 0:R] = r_.ids[...].reshape(1, R)
    r_.meta[me, 1:2, 0:48] = r_.halo[...].reshape(1, 48)
    for d in range(1, N):
        send(r_.meta.at[me], r_.meta.at[me], r_.meta_s.at[0], r_.meta_r.at[0], nodes=(me + d) % N)
    sent(r_.meta.at[0 : N - 1], r_.meta_s.at[0])
    own_rows.wait()
    gather_start(r_.xs.at[0], 0)

    src_row = r_.edge_src[...].reshape(1, E)
    src_row = jnp.where(src_row < R + 24, src_row, src_row + 8)
    dst_row = r_.edge_dst[...].reshape(1, E)
    src_col = jnp.broadcast_to(src_row, (128, E)).T[:, 0:1]
    dst_col = jnp.broadcast_to(dst_row, (128, E)).T[:, 0:1]
    as_mask = lambda cond: cond.astype(F32).astype(BF16)
    r_.T[...] = as_mask(dst_col == lax.broadcasted_iota(I32, (E, R), 1))
    r_.TT[...] = as_mask(dst_row == lax.broadcasted_iota(I32, (R, E), 0))
    r_.S[...] = as_mask(src_col == lax.broadcasted_iota(I32, (E, 256), 1))
    r_.ST[...] = as_mask(src_row == lax.broadcasted_iota(I32, (256, E), 0))
    loads[0].wait()
    r_.efT[...] = r_.ef[...].T
    loads[1].wait()
    for l in range(L):
        r_.ce[l] = dot(r_.ef[...], r_.we[l])
    r_.xf[0] = r_.xs[0, me].astype(F32)
    for load in loads[2:]:
        load.wait()

    arrive(r_.meta.at[0 : N - 1], r_.meta_r.at[0])
    id_col = jnp.broadcast_to(r_.meta[me][0:1, 0:R], (128, R)).T[:, 0:1]
    id_row = jnp.concatenate([r_.meta[j][0:1, 0:R] for j in range(N)], 1)
    r_.bias[...] = jnp.where(id_col == id_row, 0.0, NEG)

    def halo_onehot(device, start):
        row = jnp.broadcast_to(r_.meta[device][1:2, 0:128], (128, 128)).T[start : start + 24, 0:1]
        hot = (row == lax.broadcasted_iota(I32, (24, R), 1)).astype(F32)
        return jnp.concatenate([hot, jnp.zeros((8, R), F32)], 0).astype(BF16)

    r_.HP[...] = halo_onehot(prev, 24)
    r_.HN[...] = halo_onehot(nxt, 0)
    r_.A[...] = as_mask(r_.meta[me][1:2, 0:64] == lax.broadcasted_iota(I32, (R, 64), 0))

    def layer_forward(l):
        xs = r_.xs
        xb = xs[l, me]
        x = r_.xf[l]
        kv = dot(xs[l].reshape(G, D), r_.wqkv[l, :, D:])
        r_.kk[l] = kv[:, :D].astype(BF16)
        r_.vv[l] = kv[:, D:].astype(BF16)
        r_.q[l] = dot(xb, r_.wqkv[l, :, :D]).astype(BF16).astype(F32)
        r_.xe[l, 0:R] = xb
        r_.xe[l, R : R + 32] = dot(r_.HP[...], xs[l, prev]).astype(BF16)
        r_.xe[l, R + 32 : R + 64] = dot(r_.HN[...], xs[l, nxt]).astype(BF16)
        xe = r_.xe[l]
        tab_b = dot(xe, r_.wp[l, :, D : 2 * D]).astype(BF16)
        tab_e = dot(xe, r_.wp[l, :, 3 * D :]).astype(BF16)
        pa = dot(xb, r_.wp[l, :, 0:D])
        pd = dot(xb, r_.wp[l, :, 2 * D : 3 * D])
        bs = dot(r_.S[...], tab_b)
        r_.bs[l] = bs.astype(BF16)
        gate = sigmoid(select_rows(r_.T[...], pd) + dot(r_.S[...], tab_e) + r_.ce[l])
        r_.gate[l] = gate
        num = select_rows(r_.TT[...], gate * bs)
        den = select_rows(r_.TT[...], gate)
        r_.num[l] = num
        r_.den[l] = den
        msg = pa + num / (den + GATE_EPS)
        r_.z0[l] = msg
        mean0 = col_sum(msg) / R
        sq0 = col_sum((msg - mean0) * (msg - mean0))
        r_.oraw[l] = jnp.zeros((R, D), F32)
        r_.inv[l] = jnp.zeros((R, D), F32)

        def head(h, carry):
            here = lane_head == h
            qm = jnp.where(here, r_.q[l], 0.0).astype(BF16)
            s = dot_nt(qm, r_.kk[l]) + r_.bias[...]
            top = jnp.max(s, 1, keepdims=True)
            e = jnp.exp2((s - top) * (scale * math.log2(math.e)))
            inv = 1.0 / jnp.sum(e, 1, keepdims=True)
            e = e.astype(BF16)
            r_.pst[l, pl.ds(pl.multiple_of(h * R, 64), R)] = e
            o = dot(e, r_.vv[l])
            r_.oraw[l] = jnp.where(here, o * inv, r_.oraw[l])
            r_.inv[l] = jnp.where(here, jnp.broadcast_to(inv, (R, D)), r_.inv[l])
            return carry

        lax.fori_loop(0, HEADS, head, 0)
        ob = r_.oraw[l].astype(BF16)
        r_.ob[l] = ob
        t1 = x + dot(ob, r_.wo[l])
        r_.z1[l] = t1
        mean1 = col_sum(t1) / R
        sq1 = col_sum((t1 - mean1) * (t1 - mean1))
        sync_start(2 * l, pack(mean0, mean1, sq0, sq1))

    def layer_forward_rest(l):
        mean0, mean1, sq0, sq1 = sync_finish(2 * l, combine_pair)
        inv0 = lax.rsqrt(sq0 / total + NORM_EPS)
        inv1 = lax.rsqrt(sq1 / total + NORM_EPS)
        r_.iv[l, 0:1] = inv0
        r_.iv[l, 1:2] = inv1
        z0 = (r_.z0[l] - mean0) * inv0
        z1 = (r_.z1[l] - mean1) * inv1
        r_.z0[l] = z0
        r_.z1[l] = z1
        n0 = z0 * r_.gain[0, l : l + 1] + r_.shift[0, l : l + 1]
        mix = r_.xf[l] + n0 * sigmoid(n0) + z1 * r_.gain[1, l : l + 1] + r_.shift[1, l : l + 1]
        mb = mix.astype(BF16)
        r_.mb[l] = mb
        u = dot(mb, r_.wu[l])
        r_.u[l] = u
        g = (u * sigmoid(u)).astype(BF16)
        r_.g[l] = g
        return mix + dot(g, r_.wd[l])

    gather_finish(r_.xs.at[0], 0)
    zero_row = jnp.zeros((1, D), F32)
    for l in range(L):
        layer_forward(l)
        y = layer_forward_rest(l)
        r_.z2[l] = y
        mean = col_sum(y) / R
        cent = y - mean
        sq = col_sum(cent * cent)
        gain, shift = r_.gain[2, l : l + 1], r_.shift[2, l : l + 1]
        k = 2 * l + 1
        if l < L - 1:
            r_.yc[me] = cent.astype(BF16)
            sync_start(k, pack(mean, zero_row, sq, zero_row))
            gather_start(r_.yc, l + 1)
            tot_mean, _, tot_sq, _ = sync_finish(k, combine_last)
            inv2 = lax.rsqrt(tot_sq / total + NORM_EPS)
            r_.iv[l, 2:3] = inv2
            z2 = (r_.z2[l] - tot_mean) * inv2
            r_.z2[l] = z2
            r_.xf[l + 1] = z2 * gain + shift
            gather_finish(r_.yc, l + 1)
            factor = inv2 * gain
            for j in range(N):
                tile = r_.st1[k, j]
                mean_j = jnp.concatenate([tile[0:1], tile[1:2]], 1)
                moved = (r_.yc[j].astype(F32) + (mean_j - tot_mean)) * factor + shift
                r_.xs[l + 1, j] = moved.astype(BF16)
            r_.xs[l + 1, me] = r_.xf[l + 1].astype(BF16)
        else:
            dy = r_.cot[...].astype(F32)
            sync_start(k, pack(mean, col_sum(dy), sq, col_sum(dy * cent)))
            tot_mean, dy_sum, tot_sq, dy_cent = sync_finish(k, combine_last)
            inv2 = lax.rsqrt(tot_sq / total + NORM_EPS)
            r_.iv[l, 2:3] = inv2
            z2 = (r_.z2[l] - tot_mean) * inv2
            r_.z2[l] = z2
            r_.oact[...] = z2 * gain + shift
            pltpu.make_async_copy(r_.oact, r_.out_act, r_.store.at[0]).start()
            sums = (dy_sum, dy_cent * inv2)

    k_back = {1: 4, 0: 6}
    W2 = 2 * R

    def back_feed_forward(l, dy, sums):
        s2, g2 = sums
        r_.gshift[2, l : l + 1] = s2
        r_.ggain[2, l : l + 1] = g2
        d3 = r_.gain[2, l : l + 1] * r_.iv[l, 2:3] * (dy - s2 / total - r_.z2[l] * (g2 / total))
        db = d3.astype(BF16)
        dub = (dot_nt(db, r_.wd[l]) * silu_slope(r_.u[l])).astype(BF16)
        dmix = d3 + dot_nt(dub, r_.wu[l])
        r_.dmix[...] = dmix
        n0 = r_.z0[l] * r_.gain[0, l : l + 1] + r_.shift[0, l : l + 1]
        gy0 = dmix * silu_slope(n0)
        sync_start(k_back[l], pack(col_sum(dmix), col_sum(dmix * r_.z1[l]), col_sum(gy0), col_sum(gy0 * r_.z0[l])))
        base = 0 if l == L - 1 else 1280
        r_.gs1[base + 768 : base + 1280] = dot_tn(r_.g[l], db).astype(BF16)
        gu = dot_tn(r_.mb[l], dub).astype(BF16)
        r_.gs1[base + 256 : base + 512] = gu[:, 0:D]
        r_.gs1[base + 512 : base + 768] = gu[:, D:]
        q = r_.q[l]
        for h in range(HEADS):
            r_.qm[h * R : (h + 1) * R] = jnp.where(lane_head == h, q, 0.0).astype(BF16)
        r_.qmT[...] = r_.qm[...].T

    def back_norms(l):
        s1, g1, s0, g0 = sync_finish(k_back[l], combine_sum)
        r_.gshift[1, l : l + 1] = s1
        r_.ggain[1, l : l + 1] = g1
        r_.gshift[0, l : l + 1] = s0
        r_.ggain[0, l : l + 1] = g0
        dmix = r_.dmix[...]
        d2 = r_.gain[1, l : l + 1] * r_.iv[l, 1:2] * (dmix - s1 / total - r_.z1[l] * (g1 / total))
        dab = d2.astype(BF16)
        r_.dxo[...] = dmix + d2
        base = 0 if l == L - 1 else 1280
        r_.gs1[base : base + 256] = dot_tn(r_.ob[l], dab).astype(BF16)
        dob = dot_nt(dab, r_.wo[l]).astype(BF16).astype(F32)
        dos = dob * r_.inv[l]
        prod = dos * r_.oraw[l]
        for h in range(HEADS):
            here = lane_head == h
            r_.dom[h * R : (h + 1) * R] = jnp.where(here, dos, 0.0).astype(BF16)
            r_.delta[h * R : (h + 1) * R] = jnp.sum(jnp.where(here, prod, 0.0), 1, keepdims=True)
        r_.domT[...] = r_.dom[...].T

    def block_of(i):
        return (z + 1 + i) % NZ

    def back_attention(l, between):
        r_.gkv[...] = jnp.zeros((2 * D, D), F32)

        def pass_on(i):
            zb = block_of(i)
            arrive(r_.rs1.at[l, zb], r_.rsp_r.at[l, i])
            both = r_.dxs[l, zb, par].astype(F32) + r_.rs1[l, zb].astype(F32)
            r_.cs[l, zb] = both.astype(BF16)
            send(r_.cs.at[l, zb], r_.rs2.at[l, z], r_.rsc_s.at[l, i], r_.rsc_r.at[l, i], nodes=2 * zb + par)

        def block(i, carry):
            zb = block_of(i)
            cols = pl.ds(pl.multiple_of(zb * W2, 128), W2)
            for h in range(HEADS):
                rows = slice(h * R, (h + 1) * R)
                dp = dot_nt(r_.dom[rows], r_.vv[l, cols])
                ds = r_.pst[l, rows, cols].astype(F32) * (dp - r_.delta[rows])
                r_.dss[rows, cols] = ds.astype(BF16)
            dk = (dot(r_.qmT[...], r_.dss[:, cols]) * scale).astype(BF16)
            dv = dot(r_.domT[...], r_.pst[l, :, cols]).astype(BF16)
            dkv = jnp.concatenate([dk, dv], 0)
            dx = dot(r_.wqkv[l, :, D:], dkv).T
            r_.dxs[l, zb] = dx.astype(BF16).reshape(2, R, D)
            send(r_.dxs.at[l, zb, 1 - par], r_.rs1.at[l, zb], r_.rsp_s.at[l, i], r_.rsp_r.at[l, i], nodes=partner)
            r_.gkv[...] += dot(dkv, r_.xs[l, pl.ds(2 * zb, 2)].reshape(W2, D))

            @pl.when(i > 0)
            def _():
                pass_on(i - 1)

            between(i)
            return carry

        lax.fori_loop(0, NZ, block, 0)
        for i in range(NZ):
            sent(r_.dxs.at[l, i, 0], r_.rsp_s.at[l, i])
        for i in range(NZ - 1):
            sent(r_.cs.at[l, i], r_.rsc_s.at[l, i])

    def back_queries(l):
        dq = jnp.zeros((R, D), F32)
        for h in range(HEADS):
            part = dot(r_.dss[h * R : (h + 1) * R], r_.kk[l])
            dq = jnp.where(lane_head == h, part, dq)
        dqb = (dq * scale).astype(BF16)
        r_.dxo[...] += dot_nt(dqb, r_.wqkv[l, :, 0:D])
        return dqb

    def back_convolution(l):
        s0, g0 = r_.gshift[0, l : l + 1], r_.ggain[0, l : l + 1]
        inv_den = 1.0 / (r_.den[l] + GATE_EPS)
        n0 = r_.z0[l] * r_.gain[0, l : l + 1] + r_.shift[0, l : l + 1]
        gy0 = r_.dmix[...] * silu_slope(n0)
        dm = r_.gain[0, l : l + 1] * r_.iv[l, 0:1] * (gy0 - s0 / total - r_.z0[l] * (g0 / total))
        dnum = dm * inv_den
        dden = -dnum * r_.num[l] * inv_den
        dnum_e = select_rows(r_.T[...], dnum)
        dden_e = select_rows(r_.T[...], dden)
        gate = r_.gate[l]
        dgp = (dnum_e * r_.bs[l].astype(F32) + dden_e) * gate * (1.0 - gate)
        r_.dce[...] = dgp.astype(BF16)
        dpb = select_rows(r_.ST[...], dnum_e * gate).astype(BF16)
        dpe = select_rows(r_.ST[...], dgp).astype(BF16)
        dpd = select_rows(r_.TT[...], dgp).astype(BF16)
        dmb = dm.astype(BF16)
        dxe = dot_nt(dpb, r_.wp[l, :, D : 2 * D]) + dot_nt(dpe, r_.wp[l, :, 3 * D :])
        r_.hs[l, 0] = dxe[R : R + 32].astype(BF16)
        r_.hs[l, 1] = dxe[R + 32 : R + 64].astype(BF16)
        send(r_.hs.at[l, 0], r_.hr.at[l, 1], r_.hal_s.at[l, 0], r_.hal_r.at[l, 0], nodes=prev)
        send(r_.hs.at[l, 1], r_.hr.at[l, 0], r_.hal_s.at[l, 1], r_.hal_r.at[l, 1], nodes=nxt)
        sent(r_.hs.at[l, 0], r_.hal_s.at[l, 0])
        sent(r_.hs.at[l, 1], r_.hal_s.at[l, 1])
        r_.dxo[...] += (
            dxe[0:R]
            + dot_nt(dmb, r_.wp[l, :, 0:D])
            + dot_nt(dpd, r_.wp[l, :, 2 * D : 3 * D])
        )
        r_.dproj[0, 0:R] = dmb
        r_.dproj[1] = dpb
        r_.dproj[2, 0:R] = dpd
        r_.dproj[3] = dpe

    def conv_weight_grads(l, proj, at, edge, edge_at):
        r_.xeT[l] = r_.xe[l].T
        for c in range(4):
            width = R if c % 2 == 0 else 256
            made = dot(r_.xeT[l, :, 0:width], r_.dproj[c, 0:width])
            proj[at + 256 * c : at + 256 * (c + 1)] = made.astype(BF16)
        edge[edge_at : edge_at + 256] = dot(r_.efT[...], r_.dce[...]).astype(BF16)

    def back_input(l):
        dx = r_.dxo[...]
        arrive(r_.rs1.at[l, z], r_.rsp_r.at[l, NZ - 1])
        dx = dx + r_.dxs[l, z, par].astype(F32) + r_.rs1[l, z].astype(F32)
        for d in range(1, NZ):
            c = (z + NZ - d) % NZ
            arrive(r_.rs2.at[l, c], r_.rsc_r.at[l, d - 1])
            dx = dx + r_.rs2[l, c].astype(F32)
        arrive(r_.hr.at[l, 0], r_.hal_r.at[l, 1])
        arrive(r_.hr.at[l, 1], r_.hal_r.at[l, 0])
        back = jnp.concatenate(
            [r_.hr[l, 0].astype(F32)[0:24], r_.hr[l, 1].astype(F32)[0:24], jnp.zeros((16, D), F32)], 0
        )
        return dx + dot(r_.A[...], back.astype(BF16))

    back_feed_forward(1, r_.cot[...].astype(F32), sums)
    back_norms(1)
    back_attention(1, lambda i: None)
    back_convolution(1)
    dqb = back_queries(1)
    dx = back_input(1)
    r_.gin[...] = dx
    sync_start(5, pack(col_sum(dx), col_sum(dx * r_.z2[0]), zero_row, zero_row))
    conv_weight_grads(1, r_.gs0, 768, r_.gs0, 1792)
    r_.gs0[0:256] = dot(r_.xeT[1, :, 0:R], dqb).astype(BF16)
    gkv = r_.gkv[...].T.astype(BF16)
    r_.gs0[256:512] = gkv[:, 0:D]
    r_.gs0[512:768] = gkv[:, D:]
    s2, g2, _, _ = sync_finish(5, combine_sum)
    reduce_step(0, 0)

    back_feed_forward(0, r_.gin[...], (s2, g2))
    back_norms(0)
    reduce_step(1, 0)
    reduce_step(0, 1)
    back_convolution(0)
    conv_weight_grads(0, r_.gs2, 0, r_.gs4, 256)
    reduce_step(2, 0)
    reduce_step(0, 2)

    def between(i):
        @pl.when(i == 1)
        def _():
            reduce_step(1, 1)
            reduce_step(0, 3)

        @pl.when(i == 2)
        def _():
            reduce_step(2, 1)

        @pl.when(i == NZ - 1)
        def _():
            reduce_step(1, 2)

    back_attention(0, between)
    gkv = r_.gkv[...].T.astype(BF16)
    r_.gs3[256:512] = gkv[:, 0:D]
    r_.gs4[0:256] = gkv[:, D:]
    reduce_step(4, 0)
    dqb = back_queries(0)
    r_.gs3[0:256] = dot(r_.xeT[0, :, 0:R], dqb).astype(BF16)
    reduce_step(3, 0)
    reduce_step(2, 2)
    r_.gin[...] = back_input(0)
    pltpu.make_async_copy(r_.gin, r_.grad_in, r_.store.at[1]).start()
    reduce_step(3, 1)
    reduce_step(4, 1)
    reduce_step(1, 3)
    reduce_step(3, 2)
    reduce_step(4, 2)
    reduce_step(2, 3)
    reduce_step(3, 3)
    reduce_step(4, 3)
    for g in range(len(GROUPS)):
        reduce_step(g, 4)
        reduce_drain(g)
    pltpu.make_async_copy(r_.oact, r_.out_act, r_.store.at[0]).wait()
    pltpu.make_async_copy(r_.gin, r_.grad_in, r_.store.at[1]).wait()
    for src, s_sem in drains:
        remote(src, src, s_sem, s_sem, nodes=partner).wait_send()


def finish_kernel(
    act_h, gin_h, g0_h, g1_h, g2_h, g3_h, g4_h, ggain_h, gshift_h,
    act_o, gin_o, proj_o, edge_o, qkv_o, out_o, up_o, down_o, ggain_o, gshift_o,
    g0, g1, g2, g3, g4, proj, edge, qkv, out, up, down, in_sem, out_sem,
):
    direct = [
        pltpu.make_async_copy(src, dst, out_sem.at[12 + i])
        for i, (src, dst) in enumerate(((act_h, act_o), (gin_h, gin_o), (ggain_h, ggain_o), (gshift_h, gshift_o)))
    ]
    loads = [
        pltpu.make_async_copy(src, dst, in_sem.at[i])
        for i, (src, dst) in enumerate(((g0_h, g0), (g1_h, g1), (g2_h, g2), (g3_h, g3), (g4_h, g4)))
    ]
    for copy in loads + direct:
        copy.start()
    stores = []

    def store(src, dst, l):
        copy = pltpu.make_async_copy(src.at[l], dst.at[l], out_sem.at[len(stores)])
        copy.start()
        stores.append(copy)

    def widen(dst, l, src, at, count):
        for c in range(count):
            dst[l, :, 256 * c : 256 * (c + 1)] = src[at + 256 * c : at + 256 * (c + 1)].astype(F32)

    loads[0].wait()
    widen(proj, 1, g0, 768, 4)
    store(proj, proj_o, 1)
    widen(qkv, 1, g0, 0, 3)
    store(qkv, qkv_o, 1)
    widen(edge, 1, g0, 1792, 1)
    store(edge, edge_o, 1)
    loads[1].wait()
    for l, base in ((1, 0), (0, 1280)):
        widen(up, l, g1, base + 256, 2)
        store(up, up_o, l)
        down[l] = g1[base + 768 : base + 1280].astype(F32)
        store(down, down_o, l)
        widen(out, l, g1, base, 1)
        store(out, out_o, l)
    loads[2].wait()
    widen(proj, 0, g2, 0, 4)
    store(proj, proj_o, 0)
    loads[3].wait()
    loads[4].wait()
    widen(qkv, 0, g3, 0, 2)
    qkv[0, :, 512:768] = g4[0:256].astype(F32)
    store(qkv, qkv_o, 0)
    widen(edge, 0, g4, 256, 1)
    store(edge, edge_o, 0)
    for copy in stores + direct:
        copy.wait()


def fused_device(
    N, M, node_input, edge_feat, graph_ids, edge_src, edge_dst, halo_send, w_proj, w_edge, w_qkv,
    w_out, w_up, w_down, norm_gain, norm_shift, cotangent,
):
    R, D = node_input.shape
    E = edge_feat.shape[0]
    L = w_proj.shape[0]
    names = scratch_list(N, M, L, R, E)
    vmem = pl.BlockSpec(memory_space=pltpu.VMEM)
    hbm = pl.BlockSpec(memory_space=pltpu.HBM)
    shape = jax.ShapeDtypeStruct
    rows = shape((R, D), F32)
    norm = shape((3, L, D), F32)
    outs = pl.pallas_call(
        functools.partial(kernel, N, M, L, tuple(names)),
        out_shape=[rows, rows] + [shape((count, D), BF16) for count, _ in GROUPS] + [norm, norm],
        in_specs=[hbm] + [vmem] * 4 + [hbm] * 7 + [vmem] * 2 + [hbm],
        out_specs=[hbm] * (2 + len(GROUPS)) + [vmem] * 2,
        scratch_shapes=list(names.values()),
        compiler_params=pltpu.CompilerParams(
            collective_id=0, has_side_effects=True, vmem_limit_bytes=60 << 20
        ),
        name="layers",
    )(node_input, graph_ids, edge_src, edge_dst, halo_send, edge_feat, w_proj, w_edge, w_qkv, w_out, w_up,
      w_down, norm_gain.transpose(1, 0, 2), norm_shift.transpose(1, 0, 2), cotangent)
    weights = (w_proj, w_edge, w_qkv, w_out, w_up, w_down)
    results = pl.pallas_call(
        finish_kernel,
        out_shape=[rows, rows] + [shape(w.shape, F32) for w in weights] + [norm, norm],
        in_specs=[hbm] * len(outs),
        out_specs=[hbm] * 10,
        scratch_shapes=[pltpu.VMEM((count, D), BF16) for count, _ in GROUPS]
        + [pltpu.VMEM(w.shape, F32) for w in weights]
        + [pltpu.SemaphoreType.DMA((len(GROUPS),)), pltpu.SemaphoreType.DMA((16,))],
        compiler_params=pltpu.CompilerParams(vmem_limit_bytes=60 << 20),
        name="gradients",
    )(*outs)
    ggain, gshift = results[8].transpose(1, 0, 2), results[9].transpose(1, 0, 2)
    return (*results[:8], ggain, gshift)


BLOCK_CAP = 2048


def extended_2(block, sides, width):
    for axis, dim in sides:
        count = lax.axis_size(axis)
        forward = [(i, i + 1) for i in range(count - 1)]
        forward.append((count - 1, 0))
        backward = [(target, source) for source, target in forward]
        low = lax.ppermute(
            lax.slice_in_dim(block, block.shape[dim] - width, None, axis=dim), axis, forward
        )
        high = lax.ppermute(lax.slice_in_dim(block, 0, width, axis=dim), axis, backward)
        block = jnp.concatenate([low, block, high], axis=dim)
    return block


def block_length(total_rows, upper_limit):
    for length in range(min(total_rows, upper_limit), 0, -1):
        if total_rows % length == 0:
            return length
    return 1


def outer_product(left, right):
    return lax.dot_general(
        left, right, (((0,), (0,)), ((), ())), preferred_element_type=jnp.float32
    )


def times_transposed(left, weight):
    return lax.dot_general(
        left, weight, (((1,), (1,)), ((), ())), preferred_element_type=jnp.float32
    )


def forward_product(left, weight):
    return jnp.dot(left, weight, preferred_element_type=jnp.float32)


def silu_slope_plain(inputs):
    logistic = jax.nn.sigmoid(inputs)
    return logistic * (1.0 + inputs * (1.0 - logistic))


def normalize(inputs, gain_row, shift_row, node_total):
    batch_mean = lax.psum(jnp.sum(inputs, 0), ("nodes", "rep")) / node_total
    centred = inputs - batch_mean
    batch_var = lax.psum(jnp.sum(centred * centred, 0), ("nodes", "rep")) / node_total
    inv_std = lax.rsqrt(batch_var + NORM_EPS)
    standard = (inputs - batch_mean) * inv_std
    return (standard * gain_row + shift_row, standard, inv_std)


def normalize_back(grad_out, standard, inv_std, gain_row, node_total):
    shift_grad, gain_grad = lax.psum(
        (jnp.sum(grad_out, 0), jnp.sum(grad_out * standard, 0)), ("nodes", "rep")
    )
    grad_in = (
        gain_row
        * inv_std
        * (grad_out - shift_grad / node_total - standard * gain_grad / node_total)
    )
    return (grad_in, gain_grad, shift_grad)


def exchange_sources(outgoing):
    halo_rows = outgoing.shape[0] // 2
    grown = extended_2(outgoing, (("nodes", 0),), halo_rows)
    return jnp.concatenate([grown[:halo_rows], grown[3 * halo_rows :]], 0)


def return_sources(incoming_grad):
    halo_rows = incoming_grad.shape[0] // 2
    grown = extended_2(incoming_grad.astype(jnp.bfloat16), (("nodes", 0),), halo_rows).astype(
        incoming_grad.dtype
    )
    return jnp.concatenate([grown[:halo_rows], grown[3 * halo_rows :]], 0)


def attend_forward(query_rows, key_rows, value_rows, local_graphs, group_graphs):
    row_count = query_rows.shape[0]
    score_scale = HEAD_DIM ** (-0.5)
    queries = query_rows.reshape(row_count, HEADS, HEAD_DIM)

    def add_piece(carried, kv_piece, first_row):
        key_piece, value_piece = kv_piece
        piece_rows = key_piece.shape[0]
        block_len = block_length(piece_rows, BLOCK_CAP)

        def add_block(block_state, block_index):
            row_max, row_sum, accumulated = block_state
            block_start = block_index * block_len
            key_block = lax.dynamic_slice_in_dim(key_piece, block_start, block_len, 0).reshape(
                block_len, HEADS, HEAD_DIM
            )
            value_block = lax.dynamic_slice_in_dim(value_piece, block_start, block_len, 0).reshape(
                block_len, HEADS, HEAD_DIM
            )
            key_graphs = lax.dynamic_slice_in_dim(
                group_graphs, first_row + block_start, block_len, 0
            )
            same_graph = (local_graphs[:, None] == key_graphs[None, :])[None]
            scores = (
                jnp.einsum("qhd,khd->hqk", queries, key_block, preferred_element_type=jnp.float32)
                * score_scale
            )
            scores = jnp.where(same_graph, scores, NEG)
            new_max = jnp.maximum(row_max, jnp.max(scores, 2))
            weights = jnp.where(same_graph, jnp.exp(scores - new_max[:, :, None]), 0.0)
            factor = jnp.exp(row_max - new_max)
            row_sum = row_sum * factor + jnp.sum(weights, 2)
            contrib = jnp.einsum(
                "hqk,khd->qhd",
                weights.astype(jnp.bfloat16),
                value_block,
                preferred_element_type=jnp.float32,
            )
            accumulated = accumulated * jnp.transpose(factor)[:, :, None] + contrib
            return ((new_max, row_sum, accumulated), None)

        carried, _ = lax.scan(add_block, carried, jnp.arange(piece_rows // block_len))
        return carried

    start_state = (
        jnp.full((HEADS, row_count), NEG, jnp.float32),
        jnp.zeros((HEADS, row_count), jnp.float32),
        jnp.zeros((row_count, HEADS, HEAD_DIM), jnp.float32),
    )
    row_max, row_sum, accumulated = add_piece(
        start_state,
        (
            lax.all_gather(key_rows, "nodes", axis=0, tiled=True),
            lax.all_gather(value_rows, "nodes", axis=0, tiled=True),
        ),
        jnp.int32(0),
    )
    attn_raw = accumulated / jnp.transpose(row_sum)[:, :, None]
    log_sum = row_max + jnp.log(row_sum)
    return (attn_raw, log_sum)


def attend_backward(
    query_rows, key_rows, value_rows, grad_low, attn_raw, log_sum, local_graphs, group_graphs
):
    row_count = query_rows.shape[0]
    model_width = HEADS * HEAD_DIM
    score_scale = HEAD_DIM ** (-0.5)
    queries = query_rows.reshape(row_count, HEADS, HEAD_DIM)
    grad_heads = grad_low.reshape(row_count, HEADS, HEAD_DIM)
    row_delta = jnp.einsum("qhd,qhd->hq", grad_heads.astype(jnp.float32), attn_raw)

    def score_block(key_block, value_block, key_graphs):
        same_graph = (local_graphs[:, None] == key_graphs[None, :])[None]
        scores = (
            jnp.einsum("qhd,khd->hqk", queries, key_block, preferred_element_type=jnp.float32)
            * score_scale
        )
        attn_weights = jnp.exp(jnp.where(same_graph, scores - log_sum[:, :, None], NEG))
        grad_weights = jnp.einsum(
            "qhd,khd->hqk", grad_heads, value_block, preferred_element_type=jnp.float32
        )
        grad_scores = (attn_weights * (grad_weights - row_delta[:, :, None])).astype(jnp.bfloat16)
        return (attn_weights, grad_scores)

    def key_terms(attn_weights, grad_scores, block_len):
        grad_keys = (
            jnp.einsum("hqk,qhd->khd", grad_scores, queries, preferred_element_type=jnp.float32)
            * score_scale
        )
        grad_values = jnp.einsum(
            "hqk,qhd->khd",
            attn_weights.astype(jnp.bfloat16),
            grad_heads,
            preferred_element_type=jnp.float32,
        )
        return jnp.concatenate(
            [
                grad_keys.reshape(block_len, model_width),
                grad_values.reshape(block_len, model_width),
            ],
            1,
        )

    def query_term(grad_scores, key_block):
        return (
            jnp.einsum("hqk,khd->qhd", grad_scores, key_block, preferred_element_type=jnp.float32)
            * score_scale
        )

    group_rows = group_graphs.shape[0]

    def add_piece(carried, kv_piece, first_row):
        key_piece, value_piece = kv_piece
        piece_rows = key_piece.shape[0]
        block_len = block_length(piece_rows, BLOCK_CAP)

        def add_block(block_state, block_index):
            grad_query, buffer = block_state
            block_start = block_index * block_len
            key_block = lax.dynamic_slice_in_dim(key_piece, block_start, block_len, 0).reshape(
                block_len, HEADS, HEAD_DIM
            )
            value_block = lax.dynamic_slice_in_dim(value_piece, block_start, block_len, 0).reshape(
                block_len, HEADS, HEAD_DIM
            )
            place = first_row + block_start
            key_graphs = lax.dynamic_slice_in_dim(group_graphs, place, block_len, 0)
            attn_weights, grad_scores = score_block(key_block, value_block, key_graphs)
            grad_query = grad_query + query_term(grad_scores, key_block)
            block_terms = key_terms(attn_weights, grad_scores, block_len)
            current = lax.dynamic_slice_in_dim(buffer, place, block_len, 0)
            buffer = lax.dynamic_update_slice_in_dim(buffer, current + block_terms, place, 0)
            return ((grad_query, buffer), None)

        carried, _ = lax.scan(add_block, carried, jnp.arange(piece_rows // block_len))
        return carried

    start_state = (
        jnp.zeros((row_count, HEADS, HEAD_DIM), jnp.float32),
        jnp.zeros((group_rows, 2 * model_width), jnp.float32),
    )
    grad_query, buffer = add_piece(
        start_state,
        (
            lax.all_gather(key_rows, "nodes", axis=0, tiled=True),
            lax.all_gather(value_rows, "nodes", axis=0, tiled=True),
        ),
        jnp.int32(0),
    )
    grad_kv = lax.psum_scatter(buffer, "nodes", scatter_dimension=0, tiled=True)
    return (
        grad_query.reshape(row_count, model_width),
        grad_kv[:, :model_width],
        grad_kv[:, model_width:],
    )


def layer_forward(
    hidden, params, edge_feat, edge_src, edge_dst, halo_send, local_graphs, group_graphs, node_total
):
    w_proj, w_edge, w_qkv, w_out, w_up, w_down, norm_gains, norm_shifts = params
    row_count, model_width = hidden.shape
    hidden_low = hidden.astype(jnp.bfloat16)
    projected = forward_product(hidden_low, w_proj)
    self_term = projected[:, :model_width]
    dest_term = projected[:, 2 * model_width : 3 * model_width]
    source_rows = jnp.concatenate(
        [projected[:, model_width : 2 * model_width], projected[:, 3 * model_width :]], 1
    ).astype(jnp.bfloat16)
    incoming = exchange_sources(source_rows[halo_send])
    extended = jnp.concatenate([source_rows, incoming], 0)
    edge_rows = extended[edge_src].astype(jnp.float32)
    source_b = edge_rows[:, :model_width]
    source_e = edge_rows[:, model_width:]
    edge_proj = forward_product(edge_feat, w_edge)
    gating = jax.nn.sigmoid(dest_term[edge_dst] + source_e + edge_proj)
    numerator = jax.ops.segment_sum(gating * source_b, edge_dst, row_count)
    denominator = jax.ops.segment_sum(gating, edge_dst, row_count)
    message = self_term + numerator / (denominator + GATE_EPS)
    normed_one, standard_one, inv_one = normalize(
        message, norm_gains[0], norm_shifts[0], node_total
    )
    local_out = hidden + jax.nn.silu(normed_one)
    qkv_low = forward_product(hidden_low, w_qkv).astype(jnp.bfloat16)
    query_rows = qkv_low[:, :model_width]
    key_rows = qkv_low[:, model_width : 2 * model_width]
    value_rows = qkv_low[:, 2 * model_width :]
    attn_raw, log_sum = attend_forward(query_rows, key_rows, value_rows, local_graphs, group_graphs)
    attn_low = attn_raw.reshape(row_count, model_width).astype(jnp.bfloat16)
    attn_proj = forward_product(attn_low, w_out)
    normed_two, standard_two, inv_two = normalize(
        hidden + attn_proj, norm_gains[1], norm_shifts[1], node_total
    )
    mixed = local_out + normed_two
    mixed_low = mixed.astype(jnp.bfloat16)
    up_proj = forward_product(mixed_low, w_up)
    activated = jax.nn.silu(up_proj).astype(jnp.bfloat16)
    down_proj = forward_product(activated, w_down)
    normed_three, standard_three, inv_three = normalize(
        mixed + down_proj, norm_gains[2], norm_shifts[2], node_total
    )
    saved = (
        hidden_low,
        source_b,
        gating,
        numerator,
        denominator,
        normed_one,
        standard_one,
        inv_one,
        query_rows,
        key_rows,
        value_rows,
        attn_raw,
        log_sum,
        attn_low,
        standard_two,
        inv_two,
        mixed_low,
        up_proj,
        activated,
        standard_three,
        inv_three,
    )
    return (normed_three, saved)


def layer_backward(
    grad_out,
    params,
    saved,
    edge_feat,
    edge_src,
    edge_dst,
    halo_send,
    local_graphs,
    group_graphs,
    node_total,
):
    w_proj, w_edge, w_qkv, w_out, w_up, w_down, norm_gains, norm_shifts = params
    (
        hidden_low,
        source_b,
        gating,
        numerator,
        denominator,
        normed_one,
        standard_one,
        inv_one,
        query_rows,
        key_rows,
        value_rows,
        attn_raw,
        log_sum,
        attn_low,
        standard_two,
        inv_two,
        mixed_low,
        up_proj,
        activated,
        standard_three,
        inv_three,
    ) = saved
    row_count, model_width = grad_out.shape
    grad_three, gain_three, shift_three = normalize_back(
        grad_out, standard_three, inv_three, norm_gains[2], node_total
    )
    down_grad = grad_three.astype(jnp.bfloat16)
    grad_w_down = outer_product(activated, down_grad)
    up_grad = (times_transposed(down_grad, w_down) * silu_slope_plain(up_proj)).astype(jnp.bfloat16)
    grad_w_up = outer_product(mixed_low, up_grad)
    grad_mixed = grad_three + times_transposed(up_grad, w_up)
    grad_two, gain_two, shift_two = normalize_back(
        grad_mixed, standard_two, inv_two, norm_gains[1], node_total
    )
    out_grad = grad_two.astype(jnp.bfloat16)
    grad_w_out = outer_product(attn_low, out_grad)
    attn_grad = times_transposed(out_grad, w_out).astype(jnp.bfloat16)
    grad_query, grad_key, grad_value = attend_backward(
        query_rows, key_rows, value_rows, attn_grad, attn_raw, log_sum, local_graphs, group_graphs
    )
    qkv_grad = jnp.concatenate([grad_query, grad_key, grad_value], 1).astype(jnp.bfloat16)
    grad_w_qkv = outer_product(hidden_low, qkv_grad)
    grad_message, gain_one, shift_one = normalize_back(
        grad_mixed * silu_slope_plain(normed_one), standard_one, inv_one, norm_gains[0], node_total
    )
    shifted = denominator + GATE_EPS
    grad_numer = grad_message / shifted
    grad_denom = -grad_message * numerator / (shifted * shifted)
    numer_edge = grad_numer[edge_dst]
    grad_gate = numer_edge * source_b + grad_denom[edge_dst]
    grad_pre_edge = grad_gate * gating * (1.0 - gating)
    edge_grad = grad_pre_edge.astype(jnp.bfloat16)
    grad_w_edge = outer_product(edge_feat, edge_grad)
    grad_dest = jax.ops.segment_sum(grad_pre_edge, edge_dst, row_count)
    grad_extended = jax.ops.segment_sum(
        jnp.concatenate([numer_edge * gating, grad_pre_edge], 1),
        edge_src,
        row_count + halo_send.shape[0],
    )
    returned = return_sources(grad_extended[row_count:])
    grad_source = grad_extended[:row_count].at[halo_send].add(returned)
    proj_grad = jnp.concatenate(
        [grad_message, grad_source[:, :model_width], grad_dest, grad_source[:, model_width:]], 1
    ).astype(jnp.bfloat16)
    grad_w_proj = outer_product(hidden_low, proj_grad)
    grad_hidden = (
        grad_mixed
        + grad_two
        + times_transposed(proj_grad, w_proj)
        + times_transposed(qkv_grad, w_qkv)
    )
    weight_grads = (grad_w_proj, grad_w_edge, grad_w_qkv, grad_w_out, grad_w_up, grad_w_down)
    return (
        grad_hidden,
        weight_grads,
        jnp.stack([gain_one, gain_two, gain_three]),
        jnp.stack([shift_one, shift_two, shift_three]),
    )


def per_device(
    node_input,
    edge_feat,
    graph_ids,
    edge_src,
    edge_dst,
    halo_send,
    w_proj,
    w_edge,
    w_qkv,
    w_out,
    w_up,
    w_down,
    norm_gain,
    norm_shift,
    cotangent,
):
    group_graphs = lax.all_gather(graph_ids, "nodes", axis=0, tiled=True)
    node_total = node_input.shape[0] * lax.axis_size("nodes") * lax.axis_size("rep")
    layer_count = w_proj.shape[0]
    layer_params = [
        (
            w_proj[layer_index],
            w_edge[layer_index],
            w_qkv[layer_index],
            w_out[layer_index],
            w_up[layer_index],
            w_down[layer_index],
            norm_gain[layer_index],
            norm_shift[layer_index],
        )
        for layer_index in range(layer_count)
    ]
    hidden = node_input.astype(jnp.float32)
    saved_all = []
    for layer_index in range(layer_count):
        hidden, saved = layer_forward(
            hidden,
            layer_params[layer_index],
            edge_feat,
            edge_src,
            edge_dst,
            halo_send,
            graph_ids,
            group_graphs,
            node_total,
        )
        saved_all.append(saved)
    grad_hidden = cotangent.astype(jnp.float32)
    weight_parts = [None] * layer_count
    gain_parts = [None] * layer_count
    shift_parts = [None] * layer_count
    for layer_index in range(layer_count - 1, -1, -1):
        (
            grad_hidden,
            weight_parts[layer_index],
            gain_parts[layer_index],
            shift_parts[layer_index],
        ) = layer_backward(
            grad_hidden,
            layer_params[layer_index],
            saved_all[layer_index],
            edge_feat,
            edge_src,
            edge_dst,
            halo_send,
            graph_ids,
            group_graphs,
            node_total,
        )
    proj_local = jnp.stack([weight_parts[layer_index][0] for layer_index in range(layer_count)])
    edge_local = jnp.stack([weight_parts[layer_index][1] for layer_index in range(layer_count)])
    qkv_local = jnp.stack([weight_parts[layer_index][2] for layer_index in range(layer_count)])
    out_local = jnp.stack([weight_parts[layer_index][3] for layer_index in range(layer_count)])
    up_local = jnp.stack([weight_parts[layer_index][4] for layer_index in range(layer_count)])
    down_local = jnp.stack([weight_parts[layer_index][5] for layer_index in range(layer_count)])
    grad_proj, grad_edge, grad_qkv, grad_out, grad_up, grad_down = lax.psum(
        (proj_local, edge_local, qkv_local, out_local, up_local, down_local), ("nodes", "rep")
    )
    return (
        hidden,
        grad_hidden,
        grad_proj,
        grad_edge,
        grad_qkv,
        grad_out,
        grad_up,
        grad_down,
        jnp.stack(gain_parts),
        jnp.stack(shift_parts),
    )


def solution(mesh):
    in_specs = (
        P(("rep", "nodes"), None),
        P(("rep", "nodes"), None),
        P(("rep", "nodes")),
        P(("rep", "nodes")),
        P(("rep", "nodes")),
        P(("rep", "nodes")),
        P(),
        P(),
        P(),
        P(),
        P(),
        P(),
        P(),
        P(),
        P(("rep", "nodes"), None),
    )
    out_specs = (
        P(("rep", "nodes"), None),
        P(("rep", "nodes"), None),
        P(),
        P(),
        P(),
        P(),
        P(),
        P(),
        P(),
        P(),
    )
    N, M = mesh.shape["nodes"], mesh.shape["rep"]
    fused = N % 2 == 0 and N <= 8 and 512 % (16 * N * M) == 0
    return jax.shard_map(
        functools.partial(fused_device, N, M) if fused else per_device,
        mesh=mesh, in_specs=in_specs, out_specs=out_specs, check_vma=False,
    )
```

```python
import functools
import math

import jax
import jax.numpy as jnp
from jax import lax
from jax.experimental import pallas as pl
from jax.experimental.pallas import tpu as pltpu
from jax.sharding import PartitionSpec as P

HEADS = 8
HEAD_DIM = 32
NEG = -1e30
NORM_EPS = 1e-05
GATE_EPS = 1e-06
F32, BF16, I32 = jnp.float32, jnp.bfloat16, jnp.int32
MESH = pl.DeviceIdType.MESH
SYNCS = 7
GROUPS = (
    (2560, ("core", "y", "x", "z")),
    (4096, ("core", "y", "x", "z")),
    (2560, ("core", "y", "x", "z")),
    (2560, ("core", "y", "nodes")),
    (1024, ("rep", "nodes")),
    (512, ("nodes", "rep")),
)


def dot(left, right):
    return lax.dot_general(
        left, right, (((1,), (0,)), ((), ())), preferred_element_type=F32
    )


def dot_nt(left, right):
    return lax.dot_general(
        left, right, (((1,), (1,)), ((), ())), preferred_element_type=F32
    )


def dot_tn(left, right):
    return lax.dot_general(
        left, right, (((0,), (0,)), ((), ())), preferred_element_type=F32
    )


def split(value):
    high = value.astype(BF16)
    return high, (value - high.astype(F32)).astype(BF16)


def select_rows(onehot, value):
    high, low = split(value)
    return dot(onehot, high) + dot(onehot, low)


def sigmoid(value):
    return 1.0 / (1.0 + jnp.exp(-value))


def silu_slope(value):
    logistic = sigmoid(value)
    return logistic * (1.0 + value * (1.0 - logistic))


def col_sum(value):
    return jnp.sum(value, axis=0, keepdims=True)


def pack(first, second, third, fourth):
    halves = []
    for row in (first, second, third, fourth):
        halves += [row[:, :128], row[:, 128:]]
    return jnp.concatenate(halves, 0)


def unpack(tile):
    return [
        jnp.concatenate([tile[2 * i : 2 * i + 1], tile[2 * i + 1 : 2 * i + 2]], 1)
        for i in range(4)
    ]


def combine_pair(tiles, count):
    mean = jnp.mean(tiles[:, 0:4], 0)
    off = tiles[:, 0:4] - mean
    return jnp.concatenate([mean, jnp.sum(tiles[:, 4:8] + count * off * off, 0)], 0)


def combine_last(tiles, count):
    mean = jnp.mean(tiles[:, 0:2], 0)
    off = tiles[:, 0:2] - mean
    return jnp.concatenate(
        [
            mean,
            jnp.sum(tiles[:, 2:4], 0),
            jnp.sum(tiles[:, 4:6] + count * off * off, 0),
            jnp.sum(tiles[:, 6:8] + off * tiles[:, 2:4], 0),
        ],
        0,
    )


def combine_sum(tiles, count):
    return jnp.sum(tiles, 0)


class Refs:
    pass


def axis_sizes(N, M):
    return dict(core=2, y=M // 2, x=2, z=N // 2, rep=M, nodes=N)


def scratch_list(N, M, L, R, E):
    NZ, G, HR = N // 2, N * R, HEADS * R
    D, FF = 256, 512
    dma = lambda *shape: pltpu.SemaphoreType.DMA(shape)
    vm = lambda dtype, *shape: pltpu.VMEM(shape, dtype)
    names = dict(
        xs=vm(BF16, L, N, R, D),
        yc=vm(BF16, N, R, D),
        meta=vm(I32, N, 8, 256),
        ef=vm(BF16, E, D),
        cot=vm(BF16, R, D),
        wp=vm(BF16, L, D, 4 * D),
        we=vm(BF16, L, D, D),
        wqkv=vm(BF16, L, D, 3 * D),
        wo=vm(BF16, L, D, D),
        wu=vm(BF16, L, D, FF),
        wd=vm(BF16, L, FF, D),
        oact=vm(F32, R, D),
        gin=vm(F32, R, D),
        dce=vm(BF16, E, D),
        dproj=vm(BF16, 4, 256, D),
        xeT=vm(BF16, L, D, 256),
        st1=vm(F32, SYNCS, N, 8, 128),
        st2=vm(F32, SYNCS, M, 8, 128),
        T=vm(BF16, E, R),
        TT=vm(BF16, R, E),
        S=vm(BF16, E, 256),
        ST=vm(BF16, 256, E),
        efT=vm(BF16, D, E),
        HP=vm(BF16, 32, R),
        HN=vm(BF16, 32, R),
        A=vm(BF16, R, 64),
        bias=vm(F32, R, G),
        ce=vm(F32, L, E, D),
        xf=vm(F32, L, R, D),
        xe=vm(BF16, L, 256, D),
        gate=vm(F32, L, E, D),
        bs=vm(BF16, L, E, D),
        num=vm(F32, L, R, D),
        den=vm(F32, L, R, D),
        z0=vm(F32, L, R, D),
        z1=vm(F32, L, R, D),
        z2=vm(F32, L, R, D),
        q=vm(F32, L, R, D),
        kk=vm(BF16, L, G, D),
        vv=vm(BF16, L, G, D),
        pst=vm(BF16, L, HR, G),
        oraw=vm(F32, L, R, D),
        inv=vm(F32, L, R, D),
        ob=vm(BF16, L, R, D),
        mb=vm(BF16, L, R, D),
        u=vm(F32, L, R, FF),
        g=vm(BF16, L, R, FF),
        iv=vm(F32, L, 8, D),
        dmix=vm(F32, R, D),
        dxo=vm(F32, R, D),
        qm=vm(BF16, HR, D),
        qmT=vm(BF16, D, HR),
        dom=vm(BF16, HR, D),
        domT=vm(BF16, D, HR),
        delta=vm(F32, HR, 1),
        dss=vm(BF16, HR, G),
        gkv=vm(F32, 2 * D, D),
        dxs=vm(BF16, L, NZ, 2, R, D),
        rs1=vm(BF16, L, NZ, R, D),
        cs=vm(BF16, L, NZ, R, D),
        rs2=vm(BF16, L, NZ, R, D),
        hs=vm(BF16, L, 2, 32, D),
        hr=vm(BF16, L, 2, 32, D),
    )
    sizes = axis_sizes(N, M)
    for g, (rows, stages) in enumerate(GROUPS):
        names[f"gs{g}"] = vm(BF16, rows, 128)
        names[f"go{g}"] = vm(BF16, rows, 128)
        left = rows
        for k, axis in enumerate(stages):
            left //= sizes[axis]
            names[f"ga{g}_{k}"] = vm(BF16, sizes[axis] - 1, left, 128)
            if k < len(stages) - 1:
                names[f"gh{g}_{k}"] = vm(BF16, left, 128)
    names.update(
        load=dma(10),
        store=dma(2),
        meta_s=dma(1),
        meta_r=dma(1),
        st1_s=dma(SYNCS),
        st1_r=dma(SYNCS),
        st2_s=dma(SYNCS),
        st2_r=dma(SYNCS),
        agc_s=dma(L, NZ),
        agc_r=dma(L, NZ),
        agp_s=dma(L, NZ),
        agp_r=dma(L, NZ),
        rsp_s=dma(L, NZ),
        rsp_r=dma(L, NZ),
        rsc_s=dma(L, NZ),
        rsc_r=dma(L, NZ),
        hal_s=dma(L, 2),
        hal_r=dma(L, 2),
        ar_s=dma(len(GROUPS), 8),
        ar_r=dma(len(GROUPS), 8),
        ar_l=dma(len(GROUPS)),
    )
    return names


IN_NAMES = (
    "x_in", "ids", "edge_src", "edge_dst", "halo", "ef_h", "wp_h", "we_h", "wqkv_h", "wo_h", "wu_h", "wd_h",
    "gain", "shift", "cot_h",
)
OUT_NAMES = ("out_act", "grad_in", *(f"gout{g}" for g in range(len(GROUPS))), "ggain", "gshift")


def kernel(N, M, L, names, *args):
    r_ = Refs()
    for name, ref in zip(IN_NAMES + OUT_NAMES + tuple(names), args, strict=True):
        setattr(r_, name, ref)
    R, D = r_.x_in.shape
    E = r_.ef.shape[0]
    NZ, G, HR = N // 2, N * R, HEADS * R
    total = float(N * M * R)
    scale = HEAD_DIM ** -0.5
    me = lax.axis_index("nodes")
    rep = lax.axis_index("rep")
    z = me // 2
    par = me % 2
    partner = 2 * z + (1 - par)
    prev = (me + N - 1) % N
    nxt = (me + 1) % N
    drains = []

    def remote(src, dst, s_sem, r_sem, **where):
        return pltpu.make_async_remote_copy(
            src_ref=src, dst_ref=dst, send_sem=s_sem, recv_sem=r_sem,
            device_id=where, device_id_type=MESH,
        )

    def send(src, dst, s_sem, r_sem, **where):
        remote(src, dst, s_sem, r_sem, **where).start()

    def arrive(dst, r_sem):
        remote(dst, dst, r_sem, r_sem, nodes=partner).wait_recv()

    def sent(src, s_sem):
        drains.append((src, s_sem))

    loads = [
        pltpu.make_async_copy(getattr(r_, f"{name}_h"), getattr(r_, name), r_.load.at[i])
        for i, name in enumerate(("ef", "we", "wqkv", "wp", "wo", "wu", "wd", "cot"))
    ]
    own_rows = pltpu.make_async_copy(r_.x_in, r_.xs.at[0, me], r_.load.at[8])
    own_rows.start()
    for load in loads:
        load.start()

    barrier = pltpu.get_barrier_semaphore()
    for d in range(1, N):
        pl.semaphore_signal(barrier, inc=1, device_id={"nodes": (me + d) % N}, device_id_type=MESH)
    for d in range(1, M):
        pl.semaphore_signal(barrier, inc=1, device_id={"rep": (rep + d) % M}, device_id_type=MESH)
    pl.semaphore_wait(barrier, N + M - 2)

    def gather_start(buf, l):
        send(buf.at[me], buf.at[me], r_.agp_s.at[l, 0], r_.agp_r.at[l, 0], nodes=partner)
        sent(buf.at[me], r_.agp_s.at[l, 0])
        for d in range(1, NZ):
            to = 2 * ((z + d) % NZ) + par
            send(buf.at[me], buf.at[me], r_.agc_s.at[l, d], r_.agc_r.at[l, d], nodes=to)
            sent(buf.at[me], r_.agc_s.at[l, d])

    def gather_finish(buf, l):
        for d in range(1, NZ):
            c = 2 * ((z + NZ - d) % NZ) + par
            arrive(buf.at[c], r_.agc_r.at[l, d])
            send(buf.at[c], buf.at[c], r_.agp_s.at[l, d], r_.agp_r.at[l, d], nodes=partner)
            sent(buf.at[c], r_.agp_s.at[l, d])
        for d in range(NZ):
            c = 2 * ((z + NZ - d) % NZ) + 1 - par
            arrive(buf.at[c], r_.agp_r.at[l, d])

    def sync_start(k, tile):
        r_.st1[k, me] = tile
        for d in range(1, N):
            send(r_.st1.at[k, me], r_.st1.at[k, me], r_.st1_s.at[k], r_.st1_r.at[k], nodes=(me + d) % N)
        sent(r_.st1.at[k, 0 : N - 1], r_.st1_s.at[k])

    def sync_finish(k, combine):
        arrive(r_.st1.at[k, 0 : N - 1], r_.st1_r.at[k])
        r_.st2[k, rep] = combine(r_.st1[k], float(R))
        for d in range(1, M):
            send(r_.st2.at[k, rep], r_.st2.at[k, rep], r_.st2_s.at[k], r_.st2_r.at[k], rep=(rep + d) % M)
        sent(r_.st2.at[k, 0 : M - 1], r_.st2_s.at[k])
        arrive(r_.st2.at[k, 0 : M - 1], r_.st2_r.at[k])
        return unpack(combine(r_.st2[k], float(R * N)))

    sizes = axis_sizes(N, M)
    core, row = rep % 2, rep // 2
    places = dict(
        core=(core, lambda t: dict(rep=2 * row + t)),
        y=(row, lambda t: dict(rep=2 * t + core)),
        x=(par, lambda t: dict(nodes=2 * z + t)),
        z=(z, lambda t: dict(nodes=2 * t + par)),
        rep=(rep, lambda t: dict(rep=t)),
        nodes=(me, lambda t: dict(nodes=t)),
    )

    def reduce_step(g, step):
        rows, stages = GROUPS[g]
        K = len(stages)
        gs, out = getattr(r_, f"gs{g}"), getattr(r_, f"go{g}")
        count, offset = [rows], [0]
        for axis in stages:
            count.append(count[-1] // sizes[axis])
            offset.append(offset[-1] + places[axis][0] * count[-1])
        take = lambda start, size: pl.ds(pl.multiple_of(start, 16), size)
        if 1 <= step <= K:
            k = step - 1
            got = getattr(r_, f"ga{g}_{k}")
            arrive(got, r_.ar_r.at[g, k])
            held = gs if k == 0 else getattr(r_, f"gh{g}_{k - 1}")
            index = places[stages[k]][0]
            acc = held[take(index * count[k + 1], count[k + 1])].astype(F32)
            for slot in range(sizes[stages[k]] - 1):
                acc = acc + got[slot].astype(F32)
            if step < K:
                getattr(r_, f"gh{g}_{k}")[...] = acc.astype(BF16)
            else:
                out[take(offset[K], count[K])] = acc.astype(BF16)
        elif step > K:
            k = 2 * K - step
            arrive(out.at[0 : (sizes[stages[k]] - 1) * count[k + 1]], r_.ar_r.at[g, step - 1])
        if step < K:
            held = gs if step == 0 else getattr(r_, f"gh{g}_{step - 1}")
            index, device = places[stages[step]]
            size = sizes[stages[step]]
            for d in range(1, size):
                to = (index + d) % size
                send(held.at[take(to * count[step + 1], count[step + 1])], getattr(r_, f"ga{g}_{step}").at[d - 1],
                     r_.ar_s.at[g, step], r_.ar_r.at[g, step], **device(to))
        elif step < 2 * K:
            k = 2 * K - 1 - step
            index, device = places[stages[k]]
            size = sizes[stages[k]]
            here = out.at[take(offset[k + 1], count[k + 1])]
            for d in range(1, size):
                send(here, here, r_.ar_s.at[g, step], r_.ar_r.at[g, step], **device((index + d) % size))
        else:
            pltpu.make_async_copy(out, getattr(r_, f"gout{g}"), r_.ar_l.at[g]).start()

    def reduce_drain(g):
        rows, stages = GROUPS[g]
        K, left = len(stages), rows
        out = getattr(r_, f"go{g}")
        for k, axis in enumerate(stages):
            left //= sizes[axis]
            for step in (k, 2 * K - 1 - k):
                sent(out.at[0 : (sizes[axis] - 1) * left], r_.ar_s.at[g, step])
        pltpu.make_async_copy(out, getattr(r_, f"gout{g}"), r_.ar_l.at[g]).wait()

    def put(buf, at, value):
        rows = value.shape[0]
        for c in range(value.shape[1] // 128):
            buf[at : at + rows] = value[:, 128 * c : 128 * (c + 1)].astype(BF16)
            at += rows
        return at

    lane_head = lax.broadcasted_iota(I32, (R, D), 1) // HEAD_DIM

    r_.meta[me] = jnp.full((8, 256), -1, I32)
    r_.meta[me, 0:1, 0:R] = r_.ids[...].reshape(1, R)
    r_.meta[me, 1:2, 0:48] = r_.halo[...].reshape(1, 48)
    for d in range(1, N):
        send(r_.meta.at[me], r_.meta.at[me], r_.meta_s.at[0], r_.meta_r.at[0], nodes=(me + d) % N)
    sent(r_.meta.at[0 : N - 1], r_.meta_s.at[0])
    own_rows.wait()
    gather_start(r_.xs.at[0], 0)

    src_row = r_.edge_src[...].reshape(1, E)
    src_row = jnp.where(src_row < R + 24, src_row, src_row + 8)
    dst_row = r_.edge_dst[...].reshape(1, E)
    src_col = jnp.broadcast_to(src_row, (128, E)).T[:, 0:1]
    dst_col = jnp.broadcast_to(dst_row, (128, E)).T[:, 0:1]
    as_mask = lambda cond: cond.astype(F32).astype(BF16)
    r_.T[...] = as_mask(dst_col == lax.broadcasted_iota(I32, (E, R), 1))
    r_.TT[...] = as_mask(dst_row == lax.broadcasted_iota(I32, (R, E), 0))
    r_.S[...] = as_mask(src_col == lax.broadcasted_iota(I32, (E, 256), 1))
    r_.ST[...] = as_mask(src_row == lax.broadcasted_iota(I32, (256, E), 0))
    loads[0].wait()
    r_.efT[...] = r_.ef[...].T
    loads[1].wait()
    for l in range(L):
        r_.ce[l] = dot(r_.ef[...], r_.we[l])
    r_.xf[0] = r_.xs[0, me].astype(F32)
    for load in loads[2:]:
        load.wait()

    arrive(r_.meta.at[0 : N - 1], r_.meta_r.at[0])
    id_col = jnp.broadcast_to(r_.meta[me][0:1, 0:R], (128, R)).T[:, 0:1]
    id_row = jnp.concatenate([r_.meta[j][0:1, 0:R] for j in range(N)], 1)
    r_.bias[...] = jnp.where(id_col == id_row, 0.0, NEG)

    def halo_onehot(device, start):
        row = jnp.broadcast_to(r_.meta[device][1:2, 0:128], (128, 128)).T[start : start + 24, 0:1]
        hot = (row == lax.broadcasted_iota(I32, (24, R), 1)).astype(F32)
        return jnp.concatenate([hot, jnp.zeros((8, R), F32)], 0).astype(BF16)

    r_.HP[...] = halo_onehot(prev, 24)
    r_.HN[...] = halo_onehot(nxt, 0)
    r_.A[...] = as_mask(r_.meta[me][1:2, 0:64] == lax.broadcasted_iota(I32, (R, 64), 0))

    def layer_forward(l):
        xs = r_.xs
        xb = xs[l, me]
        x = r_.xf[l]
        kv = dot(xs[l].reshape(G, D), r_.wqkv[l, :, D:])
        r_.kk[l] = kv[:, :D].astype(BF16)
        r_.vv[l] = kv[:, D:].astype(BF16)
        r_.q[l] = dot(xb, r_.wqkv[l, :, :D]).astype(BF16).astype(F32)
        r_.xe[l, 0:R] = xb
        r_.xe[l, R : R + 32] = dot(r_.HP[...], xs[l, prev]).astype(BF16)
        r_.xe[l, R + 32 : R + 64] = dot(r_.HN[...], xs[l, nxt]).astype(BF16)
        xe = r_.xe[l]
        tab_b = dot(xe, r_.wp[l, :, D : 2 * D]).astype(BF16)
        tab_e = dot(xe, r_.wp[l, :, 3 * D :]).astype(BF16)
        pa = dot(xb, r_.wp[l, :, 0:D])
        pd = dot(xb, r_.wp[l, :, 2 * D : 3 * D])
        bs = dot(r_.S[...], tab_b)
        r_.bs[l] = bs.astype(BF16)
        gate = sigmoid(select_rows(r_.T[...], pd) + dot(r_.S[...], tab_e) + r_.ce[l])
        r_.gate[l] = gate
        num = select_rows(r_.TT[...], gate * bs)
        den = select_rows(r_.TT[...], gate)
        r_.num[l] = num
        r_.den[l] = den
        msg = pa + num / (den + GATE_EPS)
        r_.z0[l] = msg
        mean0 = col_sum(msg) / R
        sq0 = col_sum((msg - mean0) * (msg - mean0))
        r_.oraw[l] = jnp.zeros((R, D), F32)
        r_.inv[l] = jnp.zeros((R, D), F32)

        def head(h, carry):
            here = lane_head == h
            qm = jnp.where(here, r_.q[l], 0.0).astype(BF16)
            s = dot_nt(qm, r_.kk[l]) + r_.bias[...]
            top = jnp.max(s, 1, keepdims=True)
            e = jnp.exp2((s - top) * (scale * math.log2(math.e)))
            inv = 1.0 / jnp.sum(e, 1, keepdims=True)
            e = e.astype(BF16)
            r_.pst[l, pl.ds(pl.multiple_of(h * R, 64), R)] = e
            o = dot(e, r_.vv[l])
            r_.oraw[l] = jnp.where(here, o * inv, r_.oraw[l])
            r_.inv[l] = jnp.where(here, jnp.broadcast_to(inv, (R, D)), r_.inv[l])
            return carry

        lax.fori_loop(0, HEADS, head, 0)
        ob = r_.oraw[l].astype(BF16)
        r_.ob[l] = ob
        t1 = x + dot(ob, r_.wo[l])
        r_.z1[l] = t1
        mean1 = col_sum(t1) / R
        sq1 = col_sum((t1 - mean1) * (t1 - mean1))
        sync_start(2 * l, pack(mean0, mean1, sq0, sq1))

    def layer_forward_rest(l):
        mean0, mean1, sq0, sq1 = sync_finish(2 * l, combine_pair)
        inv0 = lax.rsqrt(sq0 / total + NORM_EPS)
        inv1 = lax.rsqrt(sq1 / total + NORM_EPS)
        r_.iv[l, 0:1] = inv0
        r_.iv[l, 1:2] = inv1
        z0 = (r_.z0[l] - mean0) * inv0
        z1 = (r_.z1[l] - mean1) * inv1
        r_.z0[l] = z0
        r_.z1[l] = z1
        n0 = z0 * r_.gain[0, l : l + 1] + r_.shift[0, l : l + 1]
        mix = r_.xf[l] + n0 * sigmoid(n0) + z1 * r_.gain[1, l : l + 1] + r_.shift[1, l : l + 1]
        mb = mix.astype(BF16)
        r_.mb[l] = mb
        u = dot(mb, r_.wu[l])
        r_.u[l] = u
        g = (u * sigmoid(u)).astype(BF16)
        r_.g[l] = g
        return mix + dot(g, r_.wd[l])

    gather_finish(r_.xs.at[0], 0)
    zero_row = jnp.zeros((1, D), F32)
    for l in range(L):
        layer_forward(l)
        y = layer_forward_rest(l)
        r_.z2[l] = y
        mean = col_sum(y) / R
        cent = y - mean
        sq = col_sum(cent * cent)
        gain, shift = r_.gain[2, l : l + 1], r_.shift[2, l : l + 1]
        k = 2 * l + 1
        if l < L - 1:
            r_.yc[me] = cent.astype(BF16)
            sync_start(k, pack(mean, zero_row, sq, zero_row))
            gather_start(r_.yc, l + 1)
            tot_mean, _, tot_sq, _ = sync_finish(k, combine_last)
            inv2 = lax.rsqrt(tot_sq / total + NORM_EPS)
            r_.iv[l, 2:3] = inv2
            z2 = (r_.z2[l] - tot_mean) * inv2
            r_.z2[l] = z2
            r_.xf[l + 1] = z2 * gain + shift
            gather_finish(r_.yc, l + 1)
            factor = inv2 * gain
            for j in range(N):
                tile = r_.st1[k, j]
                mean_j = jnp.concatenate([tile[0:1], tile[1:2]], 1)
                moved = (r_.yc[j].astype(F32) + (mean_j - tot_mean)) * factor + shift
                r_.xs[l + 1, j] = moved.astype(BF16)
            r_.xs[l + 1, me] = r_.xf[l + 1].astype(BF16)
        else:
            dy = r_.cot[...].astype(F32)
            sync_start(k, pack(mean, col_sum(dy), sq, col_sum(dy * cent)))
            tot_mean, dy_sum, tot_sq, dy_cent = sync_finish(k, combine_last)
            inv2 = lax.rsqrt(tot_sq / total + NORM_EPS)
            r_.iv[l, 2:3] = inv2
            z2 = (r_.z2[l] - tot_mean) * inv2
            r_.z2[l] = z2
            r_.oact[...] = z2 * gain + shift
            pltpu.make_async_copy(r_.oact, r_.out_act, r_.store.at[0]).start()
            sums = (dy_sum, dy_cent * inv2)

    k_back = {1: 4, 0: 6}
    W2 = 2 * R

    def back_feed_forward(l, dy, sums):
        s2, g2 = sums
        r_.gshift[2, l : l + 1] = s2
        r_.ggain[2, l : l + 1] = g2
        d3 = r_.gain[2, l : l + 1] * r_.iv[l, 2:3] * (dy - s2 / total - r_.z2[l] * (g2 / total))
        db = d3.astype(BF16)
        dub = (dot_nt(db, r_.wd[l]) * silu_slope(r_.u[l])).astype(BF16)
        dmix = d3 + dot_nt(dub, r_.wu[l])
        r_.dmix[...] = dmix
        n0 = r_.z0[l] * r_.gain[0, l : l + 1] + r_.shift[0, l : l + 1]
        gy0 = dmix * silu_slope(n0)
        sync_start(k_back[l], pack(col_sum(dmix), col_sum(dmix * r_.z1[l]), col_sum(gy0), col_sum(gy0 * r_.z0[l])))
        early = r_.gs0 if l == L - 1 else r_.gs2
        at = put(early, 512, dot_tn(r_.mb[l], dub))
        put(early, at, dot_tn(r_.g[l], db))
        q = r_.q[l]
        for h in range(HEADS):
            r_.qm[h * R : (h + 1) * R] = jnp.where(lane_head == h, q, 0.0).astype(BF16)
        r_.qmT[...] = r_.qm[...].T

    def back_norms(l):
        s1, g1, s0, g0 = sync_finish(k_back[l], combine_sum)
        r_.gshift[1, l : l + 1] = s1
        r_.ggain[1, l : l + 1] = g1
        r_.gshift[0, l : l + 1] = s0
        r_.ggain[0, l : l + 1] = g0
        dmix = r_.dmix[...]
        d2 = r_.gain[1, l : l + 1] * r_.iv[l, 1:2] * (dmix - s1 / total - r_.z1[l] * (g1 / total))
        dab = d2.astype(BF16)
        r_.dxo[...] = dmix + d2
        put(r_.gs0 if l == L - 1 else r_.gs2, 0, dot_tn(r_.ob[l], dab))
        dob = dot_nt(dab, r_.wo[l]).astype(BF16).astype(F32)
        dos = dob * r_.inv[l]
        prod = dos * r_.oraw[l]
        for h in range(HEADS):
            here = lane_head == h
            r_.dom[h * R : (h + 1) * R] = jnp.where(here, dos, 0.0).astype(BF16)
            r_.delta[h * R : (h + 1) * R] = jnp.sum(jnp.where(here, prod, 0.0), 1, keepdims=True)
        r_.domT[...] = r_.dom[...].T

    def block_of(i):
        return (z + 1 + i) % NZ

    def back_attention(l, between):
        r_.gkv[...] = jnp.zeros((2 * D, D), F32)

        def pass_on(i):
            zb = block_of(i)
            arrive(r_.rs1.at[l, zb], r_.rsp_r.at[l, i])
            both = r_.dxs[l, zb, par].astype(F32) + r_.rs1[l, zb].astype(F32)
            r_.cs[l, zb] = both.astype(BF16)
            send(r_.cs.at[l, zb], r_.rs2.at[l, z], r_.rsc_s.at[l, i], r_.rsc_r.at[l, i], nodes=2 * zb + par)

        def block(i, carry):
            zb = block_of(i)
            cols = pl.ds(pl.multiple_of(zb * W2, 128), W2)
            for h in range(HEADS):
                rows = slice(h * R, (h + 1) * R)
                dp = dot_nt(r_.dom[rows], r_.vv[l, cols])
                ds = r_.pst[l, rows, cols].astype(F32) * (dp - r_.delta[rows])
                r_.dss[rows, cols] = ds.astype(BF16)
            dk = (dot(r_.qmT[...], r_.dss[:, cols]) * scale).astype(BF16)
            dv = dot(r_.domT[...], r_.pst[l, :, cols]).astype(BF16)
            dkv = jnp.concatenate([dk, dv], 0)
            dx = dot(r_.wqkv[l, :, D:], dkv).T
            r_.dxs[l, zb] = dx.astype(BF16).reshape(2, R, D)
            send(r_.dxs.at[l, zb, 1 - par], r_.rs1.at[l, zb], r_.rsp_s.at[l, i], r_.rsp_r.at[l, i], nodes=partner)
            r_.gkv[...] += dot(dkv, r_.xs[l, pl.ds(2 * zb, 2)].reshape(W2, D))

            @pl.when(i > 0)
            def _():
                pass_on(i - 1)

            between(i)
            return carry

        lax.fori_loop(0, NZ, block, 0)
        for i in range(NZ):
            sent(r_.dxs.at[l, i, 0], r_.rsp_s.at[l, i])
        for i in range(NZ - 1):
            sent(r_.cs.at[l, i], r_.rsc_s.at[l, i])

    def back_queries(l):
        r_.xeT[l] = r_.xe[l].T
        dq = jnp.zeros((R, D), F32)
        for h in range(HEADS):
            part = dot(r_.dss[h * R : (h + 1) * R], r_.kk[l])
            dq = jnp.where(lane_head == h, part, dq)
        dqb = (dq * scale).astype(BF16)
        r_.dxo[...] += dot_nt(dqb, r_.wqkv[l, :, 0:D])
        return dqb

    def back_convolution(l):
        s0, g0 = r_.gshift[0, l : l + 1], r_.ggain[0, l : l + 1]
        inv_den = 1.0 / (r_.den[l] + GATE_EPS)
        n0 = r_.z0[l] * r_.gain[0, l : l + 1] + r_.shift[0, l : l + 1]
        gy0 = r_.dmix[...] * silu_slope(n0)
        dm = r_.gain[0, l : l + 1] * r_.iv[l, 0:1] * (gy0 - s0 / total - r_.z0[l] * (g0 / total))
        dnum = dm * inv_den
        dden = -dnum * r_.num[l] * inv_den
        dnum_e = select_rows(r_.T[...], dnum)
        dden_e = select_rows(r_.T[...], dden)
        gate = r_.gate[l]
        dgp = (dnum_e * r_.bs[l].astype(F32) + dden_e) * gate * (1.0 - gate)
        r_.dce[...] = dgp.astype(BF16)
        dpb = select_rows(r_.ST[...], dnum_e * gate).astype(BF16)
        dpe = select_rows(r_.ST[...], dgp).astype(BF16)
        dpd = select_rows(r_.TT[...], dgp).astype(BF16)
        dmb = dm.astype(BF16)
        dxe = dot_nt(dpb, r_.wp[l, :, D : 2 * D]) + dot_nt(dpe, r_.wp[l, :, 3 * D :])
        r_.hs[l, 0] = dxe[R : R + 32].astype(BF16)
        r_.hs[l, 1] = dxe[R + 32 : R + 64].astype(BF16)
        send(r_.hs.at[l, 0], r_.hr.at[l, 1], r_.hal_s.at[l, 0], r_.hal_r.at[l, 0], nodes=prev)
        send(r_.hs.at[l, 1], r_.hr.at[l, 0], r_.hal_s.at[l, 1], r_.hal_r.at[l, 1], nodes=nxt)
        sent(r_.hs.at[l, 0], r_.hal_s.at[l, 0])
        sent(r_.hs.at[l, 1], r_.hal_s.at[l, 1])
        r_.dxo[...] += (
            dxe[0:R]
            + dot_nt(dmb, r_.wp[l, :, 0:D])
            + dot_nt(dpd, r_.wp[l, :, 2 * D : 3 * D])
        )
        r_.dproj[0, 0:R] = dmb
        r_.dproj[1] = dpb
        r_.dproj[2, 0:R] = dpd
        r_.dproj[3] = dpe

    def conv_weight_grads(l, buf, at):
        for c in range(4):
            width = R if c % 2 == 0 else 256
            at = put(buf, at, dot(r_.xeT[l, :, 0:width], r_.dproj[c, 0:width]))
        put(buf, at, dot(r_.efT[...], r_.dce[...]))

    def back_input(l):
        dx = r_.dxo[...]
        arrive(r_.rs1.at[l, z], r_.rsp_r.at[l, NZ - 1])
        dx = dx + r_.dxs[l, z, par].astype(F32) + r_.rs1[l, z].astype(F32)
        for d in range(1, NZ):
            c = (z + NZ - d) % NZ
            arrive(r_.rs2.at[l, c], r_.rsc_r.at[l, d - 1])
            dx = dx + r_.rs2[l, c].astype(F32)
        arrive(r_.hr.at[l, 0], r_.hal_r.at[l, 1])
        arrive(r_.hr.at[l, 1], r_.hal_r.at[l, 0])
        back = jnp.concatenate(
            [r_.hr[l, 0].astype(F32)[0:24], r_.hr[l, 1].astype(F32)[0:24], jnp.zeros((16, D), F32)], 0
        )
        return dx + dot(r_.A[...], back.astype(BF16))

    back_feed_forward(1, r_.cot[...].astype(F32), sums)
    back_norms(1)
    reduce_step(0, 0)

    def between_1(i):
        for step in range(1, NZ):
            @pl.when(i == step)
            def _():
                reduce_step(0, step)

    back_attention(1, between_1)
    back_convolution(1)
    reduce_step(0, NZ)
    dqb = back_queries(1)
    dx = back_input(1)
    r_.gin[...] = dx
    sync_start(5, pack(col_sum(dx), col_sum(dx * r_.z2[0]), zero_row, zero_row))
    at = put(r_.gs1, 0, dot(r_.xeT[1, :, 0:R], dqb))
    at = put(r_.gs1, at, r_.gkv[...].T)
    conv_weight_grads(1, r_.gs1, at)
    s2, g2, _, _ = sync_finish(5, combine_sum)
    reduce_step(1, 0)

    back_feed_forward(0, r_.gin[...], (s2, g2))
    back_norms(0)
    reduce_step(1, 1)
    reduce_step(2, 0)
    reduce_step(0, 5)
    back_convolution(0)
    reduce_step(2, 1)
    reduce_step(0, 6)
    r_.xeT[0] = r_.xe[0].T
    conv_weight_grads(0, r_.gs3, 0)
    reduce_step(3, 0)
    reduce_step(1, 2)

    def between_0(i):
        @pl.when(i == 0)
        def _():
            reduce_step(0, 7)
            reduce_step(2, 2)

        @pl.when(i == 1)
        def _():
            reduce_step(1, 3)
            reduce_step(3, 1)

        @pl.when(i == 2)
        def _():
            reduce_step(2, 3)
            reduce_step(1, 4)

        @pl.when(i == NZ - 1)
        def _():
            reduce_step(3, 2)
            reduce_step(2, 4)
            reduce_step(1, 5)

    back_attention(0, between_0)
    at = put(r_.gs4, 512, r_.gkv[0:D, :].T)
    put(r_.gs5, 0, r_.gkv[D:, :].T)
    reduce_step(5, 0)
    dqb = back_queries(0)
    put(r_.gs4, 0, dot(r_.xeT[0, :, 0:R], dqb))
    reduce_step(4, 0)
    reduce_step(3, 3)
    reduce_step(2, 5)
    reduce_step(1, 6)
    r_.gin[...] = back_input(0)
    pltpu.make_async_copy(r_.gin, r_.grad_in, r_.store.at[1]).start()
    reduce_step(5, 1)
    reduce_step(4, 1)
    reduce_step(3, 4)
    reduce_step(2, 6)
    reduce_step(1, 7)
    reduce_step(5, 2)
    reduce_step(4, 2)
    reduce_step(3, 5)
    reduce_step(2, 7)
    reduce_step(0, 8)
    reduce_step(1, 8)
    reduce_step(5, 3)
    reduce_step(4, 3)
    reduce_step(3, 6)
    reduce_step(2, 8)
    reduce_step(5, 4)
    reduce_step(4, 4)
    for g in range(len(GROUPS)):
        reduce_drain(g)
    pltpu.make_async_copy(r_.oact, r_.out_act, r_.store.at[0]).wait()
    pltpu.make_async_copy(r_.gin, r_.grad_in, r_.store.at[1]).wait()
    for src, s_sem in drains:
        remote(src, src, s_sem, s_sem, nodes=partner).wait_send()


def finish_kernel(act_h, gin_h, *refs):
    n = len(GROUPS)
    held, (ggain_h, gshift_h), refs = refs[:n], refs[n : n + 2], refs[n + 2 :]
    act_o, gin_o, proj_o, edge_o, qkv_o, out_o, up_o, down_o, ggain_o, gshift_o = refs[:10]
    summed, refs = refs[10 : 10 + n], refs[10 + n :]
    act, gin, proj, edge, qkv, out, up, down, in_sem, out_sem = refs
    loads = [
        pltpu.make_async_copy(src, dst, in_sem.at[i])
        for i, (src, dst) in enumerate(zip(held + (act_h, gin_h), summed + (act, gin), strict=True))
    ]
    for i in (1, 0, 2, 3, n, n + 1, 4, 5):
        loads[i].start()
    ggain_o[...] = ggain_h[...]
    gshift_o[...] = gshift_h[...]
    stores = []

    def store(src, dst):
        copy = pltpu.make_async_copy(src, dst, out_sem.at[len(stores)])
        copy.start()
        stores.append(copy)

    def widen(dst, l, g, at, first=0, last=None):
        rows = dst.shape[1]
        for c in range(first, dst.shape[2] // 128 if last is None else last):
            dst[l, :, 128 * c : 128 * (c + 1)] = summed[g][at : at + rows].astype(F32)
            at += rows
        return at

    loads[1].wait()
    at = widen(qkv, 1, 1, 0)
    store(qkv.at[1], qkv_o.at[1])
    at = widen(proj, 1, 1, at)
    store(proj.at[1], proj_o.at[1])
    widen(edge, 1, 1, at)
    store(edge.at[1], edge_o.at[1])
    for l, g in ((1, 0), (0, 2)):
        loads[g].wait()
        at = widen(out, l, g, 0)
        store(out.at[l], out_o.at[l])
        at = widen(up, l, g, at)
        store(up.at[l], up_o.at[l])
        widen(down, l, g, at)
        store(down.at[l], down_o.at[l])
    loads[3].wait()
    at = widen(proj, 0, 3, 0)
    store(proj.at[0], proj_o.at[0])
    widen(edge, 0, 3, at)
    store(edge.at[0], edge_o.at[0])
    loads[n].wait()
    store(act, act_o)
    loads[n + 1].wait()
    store(gin, gin_o)
    loads[4].wait()
    widen(qkv, 0, 4, 0, 0, 4)
    loads[5].wait()
    widen(qkv, 0, 5, 0, 4, 6)
    store(qkv.at[0], qkv_o.at[0])
    for copy in stores:
        copy.wait()


def fused_device(
    N, M, node_input, edge_feat, graph_ids, edge_src, edge_dst, halo_send, w_proj, w_edge, w_qkv,
    w_out, w_up, w_down, norm_gain, norm_shift, cotangent,
):
    R, D = node_input.shape
    E = edge_feat.shape[0]
    L = w_proj.shape[0]
    names = scratch_list(N, M, L, R, E)
    vmem = pl.BlockSpec(memory_space=pltpu.VMEM)
    hbm = pl.BlockSpec(memory_space=pltpu.HBM)
    shape = jax.ShapeDtypeStruct
    rows = shape((R, D), F32)
    norm = shape((3, L, D), F32)
    groups = [shape((count, 128), BF16) for count, _ in GROUPS]
    outs = pl.pallas_call(
        functools.partial(kernel, N, M, L, tuple(names)),
        out_shape=[rows, rows, *groups, norm, norm],
        in_specs=[hbm] + [vmem] * 4 + [hbm] * 7 + [vmem] * 2 + [hbm],
        out_specs=[hbm] * (2 + len(GROUPS)) + [vmem] * 2,
        scratch_shapes=list(names.values()),
        compiler_params=pltpu.CompilerParams(
            collective_id=0, has_side_effects=True, vmem_limit_bytes=60 << 20
        ),
        name="layers",
    )(node_input, graph_ids, edge_src, edge_dst, halo_send, edge_feat, w_proj, w_edge, w_qkv, w_out, w_up,
      w_down, norm_gain.transpose(1, 0, 2), norm_shift.transpose(1, 0, 2), cotangent)
    weights = [shape(w.shape, F32) for w in (w_proj, w_edge, w_qkv, w_out, w_up, w_down)]
    results = pl.pallas_call(
        finish_kernel,
        out_shape=[rows, rows, *weights, norm, norm],
        in_specs=[hbm] * (2 + len(GROUPS)) + [vmem] * 2,
        out_specs=[hbm] * 8 + [vmem] * 2,
        scratch_shapes=[pltpu.VMEM(s.shape, s.dtype) for s in (*groups, rows, rows, *weights)]
        + [pltpu.SemaphoreType.DMA((len(GROUPS) + 2,)), pltpu.SemaphoreType.DMA((14,))],
        compiler_params=pltpu.CompilerParams(vmem_limit_bytes=60 << 20),
        name="gradients",
    )(*outs)
    ggain, gshift = results[8].transpose(1, 0, 2), results[9].transpose(1, 0, 2)
    return (*results[:8], ggain, gshift)


BLOCK_CAP = 2048


def extended_2(block, sides, width):
    for axis, dim in sides:
        count = lax.axis_size(axis)
        forward = [(i, i + 1) for i in range(count - 1)]
        forward.append((count - 1, 0))
        backward = [(target, source) for source, target in forward]
        low = lax.ppermute(
            lax.slice_in_dim(block, block.shape[dim] - width, None, axis=dim), axis, forward
        )
        high = lax.ppermute(lax.slice_in_dim(block, 0, width, axis=dim), axis, backward)
        block = jnp.concatenate([low, block, high], axis=dim)
    return block


def block_length(total_rows, upper_limit):
    for length in range(min(total_rows, upper_limit), 0, -1):
        if total_rows % length == 0:
            return length
    return 1


def outer_product(left, right):
    return lax.dot_general(
        left, right, (((0,), (0,)), ((), ())), preferred_element_type=jnp.float32
    )


def times_transposed(left, weight):
    return lax.dot_general(
        left, weight, (((1,), (1,)), ((), ())), preferred_element_type=jnp.float32
    )


def forward_product(left, weight):
    return jnp.dot(left, weight, preferred_element_type=jnp.float32)


def silu_slope_plain(inputs):
    logistic = jax.nn.sigmoid(inputs)
    return logistic * (1.0 + inputs * (1.0 - logistic))


def normalize(inputs, gain_row, shift_row, node_total):
    batch_mean = lax.psum(jnp.sum(inputs, 0), ("nodes", "rep")) / node_total
    centred = inputs - batch_mean
    batch_var = lax.psum(jnp.sum(centred * centred, 0), ("nodes", "rep")) / node_total
    inv_std = lax.rsqrt(batch_var + NORM_EPS)
    standard = (inputs - batch_mean) * inv_std
    return (standard * gain_row + shift_row, standard, inv_std)


def normalize_back(grad_out, standard, inv_std, gain_row, node_total):
    shift_grad, gain_grad = lax.psum(
        (jnp.sum(grad_out, 0), jnp.sum(grad_out * standard, 0)), ("nodes", "rep")
    )
    grad_in = (
        gain_row
        * inv_std
        * (grad_out - shift_grad / node_total - standard * gain_grad / node_total)
    )
    return (grad_in, gain_grad, shift_grad)


def exchange_sources(outgoing):
    halo_rows = outgoing.shape[0] // 2
    grown = extended_2(outgoing, (("nodes", 0),), halo_rows)
    return jnp.concatenate([grown[:halo_rows], grown[3 * halo_rows :]], 0)


def return_sources(incoming_grad):
    halo_rows = incoming_grad.shape[0] // 2
    grown = extended_2(incoming_grad.astype(jnp.bfloat16), (("nodes", 0),), halo_rows).astype(
        incoming_grad.dtype
    )
    return jnp.concatenate([grown[:halo_rows], grown[3 * halo_rows :]], 0)


def attend_forward(query_rows, key_rows, value_rows, local_graphs, group_graphs):
    row_count = query_rows.shape[0]
    score_scale = HEAD_DIM ** (-0.5)
    queries = query_rows.reshape(row_count, HEADS, HEAD_DIM)

    def add_piece(carried, kv_piece, first_row):
        key_piece, value_piece = kv_piece
        piece_rows = key_piece.shape[0]
        block_len = block_length(piece_rows, BLOCK_CAP)

        def add_block(block_state, block_index):
            row_max, row_sum, accumulated = block_state
            block_start = block_index * block_len
            key_block = lax.dynamic_slice_in_dim(key_piece, block_start, block_len, 0).reshape(
                block_len, HEADS, HEAD_DIM
            )
            value_block = lax.dynamic_slice_in_dim(value_piece, block_start, block_len, 0).reshape(
                block_len, HEADS, HEAD_DIM
            )
            key_graphs = lax.dynamic_slice_in_dim(
                group_graphs, first_row + block_start, block_len, 0
            )
            same_graph = (local_graphs[:, None] == key_graphs[None, :])[None]
            scores = (
                jnp.einsum("qhd,khd->hqk", queries, key_block, preferred_element_type=jnp.float32)
                * score_scale
            )
            scores = jnp.where(same_graph, scores, NEG)
            new_max = jnp.maximum(row_max, jnp.max(scores, 2))
            weights = jnp.where(same_graph, jnp.exp(scores - new_max[:, :, None]), 0.0)
            factor = jnp.exp(row_max - new_max)
            row_sum = row_sum * factor + jnp.sum(weights, 2)
            contrib = jnp.einsum(
                "hqk,khd->qhd",
                weights.astype(jnp.bfloat16),
                value_block,
                preferred_element_type=jnp.float32,
            )
            accumulated = accumulated * jnp.transpose(factor)[:, :, None] + contrib
            return ((new_max, row_sum, accumulated), None)

        carried, _ = lax.scan(add_block, carried, jnp.arange(piece_rows // block_len))
        return carried

    start_state = (
        jnp.full((HEADS, row_count), NEG, jnp.float32),
        jnp.zeros((HEADS, row_count), jnp.float32),
        jnp.zeros((row_count, HEADS, HEAD_DIM), jnp.float32),
    )
    row_max, row_sum, accumulated = add_piece(
        start_state,
        (
            lax.all_gather(key_rows, "nodes", axis=0, tiled=True),
            lax.all_gather(value_rows, "nodes", axis=0, tiled=True),
        ),
        jnp.int32(0),
    )
    attn_raw = accumulated / jnp.transpose(row_sum)[:, :, None]
    log_sum = row_max + jnp.log(row_sum)
    return (attn_raw, log_sum)


def attend_backward(
    query_rows, key_rows, value_rows, grad_low, attn_raw, log_sum, local_graphs, group_graphs
):
    row_count = query_rows.shape[0]
    model_width = HEADS * HEAD_DIM
    score_scale = HEAD_DIM ** (-0.5)
    queries = query_rows.reshape(row_count, HEADS, HEAD_DIM)
    grad_heads = grad_low.reshape(row_count, HEADS, HEAD_DIM)
    row_delta = jnp.einsum("qhd,qhd->hq", grad_heads.astype(jnp.float32), attn_raw)

    def score_block(key_block, value_block, key_graphs):
        same_graph = (local_graphs[:, None] == key_graphs[None, :])[None]
        scores = (
            jnp.einsum("qhd,khd->hqk", queries, key_block, preferred_element_type=jnp.float32)
            * score_scale
        )
        attn_weights = jnp.exp(jnp.where(same_graph, scores - log_sum[:, :, None], NEG))
        grad_weights = jnp.einsum(
            "qhd,khd->hqk", grad_heads, value_block, preferred_element_type=jnp.float32
        )
        grad_scores = (attn_weights * (grad_weights - row_delta[:, :, None])).astype(jnp.bfloat16)
        return (attn_weights, grad_scores)

    def key_terms(attn_weights, grad_scores, block_len):
        grad_keys = (
            jnp.einsum("hqk,qhd->khd", grad_scores, queries, preferred_element_type=jnp.float32)
            * score_scale
        )
        grad_values = jnp.einsum(
            "hqk,qhd->khd",
            attn_weights.astype(jnp.bfloat16),
            grad_heads,
            preferred_element_type=jnp.float32,
        )
        return jnp.concatenate(
            [
                grad_keys.reshape(block_len, model_width),
                grad_values.reshape(block_len, model_width),
            ],
            1,
        )

    def query_term(grad_scores, key_block):
        return (
            jnp.einsum("hqk,khd->qhd", grad_scores, key_block, preferred_element_type=jnp.float32)
            * score_scale
        )

    group_rows = group_graphs.shape[0]

    def add_piece(carried, kv_piece, first_row):
        key_piece, value_piece = kv_piece
        piece_rows = key_piece.shape[0]
        block_len = block_length(piece_rows, BLOCK_CAP)

        def add_block(block_state, block_index):
            grad_query, buffer = block_state
            block_start = block_index * block_len
            key_block = lax.dynamic_slice_in_dim(key_piece, block_start, block_len, 0).reshape(
                block_len, HEADS, HEAD_DIM
            )
            value_block = lax.dynamic_slice_in_dim(value_piece, block_start, block_len, 0).reshape(
                block_len, HEADS, HEAD_DIM
            )
            place = first_row + block_start
            key_graphs = lax.dynamic_slice_in_dim(group_graphs, place, block_len, 0)
            attn_weights, grad_scores = score_block(key_block, value_block, key_graphs)
            grad_query = grad_query + query_term(grad_scores, key_block)
            block_terms = key_terms(attn_weights, grad_scores, block_len)
            current = lax.dynamic_slice_in_dim(buffer, place, block_len, 0)
            buffer = lax.dynamic_update_slice_in_dim(buffer, current + block_terms, place, 0)
            return ((grad_query, buffer), None)

        carried, _ = lax.scan(add_block, carried, jnp.arange(piece_rows // block_len))
        return carried

    start_state = (
        jnp.zeros((row_count, HEADS, HEAD_DIM), jnp.float32),
        jnp.zeros((group_rows, 2 * model_width), jnp.float32),
    )
    grad_query, buffer = add_piece(
        start_state,
        (
            lax.all_gather(key_rows, "nodes", axis=0, tiled=True),
            lax.all_gather(value_rows, "nodes", axis=0, tiled=True),
        ),
        jnp.int32(0),
    )
    grad_kv = lax.psum_scatter(buffer, "nodes", scatter_dimension=0, tiled=True)
    return (
        grad_query.reshape(row_count, model_width),
        grad_kv[:, :model_width],
        grad_kv[:, model_width:],
    )


def layer_forward(
    hidden, params, edge_feat, edge_src, edge_dst, halo_send, local_graphs, group_graphs, node_total
):
    w_proj, w_edge, w_qkv, w_out, w_up, w_down, norm_gains, norm_shifts = params
    row_count, model_width = hidden.shape
    hidden_low = hidden.astype(jnp.bfloat16)
    projected = forward_product(hidden_low, w_proj)
    self_term = projected[:, :model_width]
    dest_term = projected[:, 2 * model_width : 3 * model_width]
    source_rows = jnp.concatenate(
        [projected[:, model_width : 2 * model_width], projected[:, 3 * model_width :]], 1
    ).astype(jnp.bfloat16)
    incoming = exchange_sources(source_rows[halo_send])
    extended = jnp.concatenate([source_rows, incoming], 0)
    edge_rows = extended[edge_src].astype(jnp.float32)
    source_b = edge_rows[:, :model_width]
    source_e = edge_rows[:, model_width:]
    edge_proj = forward_product(edge_feat, w_edge)
    gating = jax.nn.sigmoid(dest_term[edge_dst] + source_e + edge_proj)
    numerator = jax.ops.segment_sum(gating * source_b, edge_dst, row_count)
    denominator = jax.ops.segment_sum(gating, edge_dst, row_count)
    message = self_term + numerator / (denominator + GATE_EPS)
    normed_one, standard_one, inv_one = normalize(
        message, norm_gains[0], norm_shifts[0], node_total
    )
    local_out = hidden + jax.nn.silu(normed_one)
    qkv_low = forward_product(hidden_low, w_qkv).astype(jnp.bfloat16)
    query_rows = qkv_low[:, :model_width]
    key_rows = qkv_low[:, model_width : 2 * model_width]
    value_rows = qkv_low[:, 2 * model_width :]
    attn_raw, log_sum = attend_forward(query_rows, key_rows, value_rows, local_graphs, group_graphs)
    attn_low = attn_raw.reshape(row_count, model_width).astype(jnp.bfloat16)
    attn_proj = forward_product(attn_low, w_out)
    normed_two, standard_two, inv_two = normalize(
        hidden + attn_proj, norm_gains[1], norm_shifts[1], node_total
    )
    mixed = local_out + normed_two
    mixed_low = mixed.astype(jnp.bfloat16)
    up_proj = forward_product(mixed_low, w_up)
    activated = jax.nn.silu(up_proj).astype(jnp.bfloat16)
    down_proj = forward_product(activated, w_down)
    normed_three, standard_three, inv_three = normalize(
        mixed + down_proj, norm_gains[2], norm_shifts[2], node_total
    )
    saved = (
        hidden_low,
        source_b,
        gating,
        numerator,
        denominator,
        normed_one,
        standard_one,
        inv_one,
        query_rows,
        key_rows,
        value_rows,
        attn_raw,
        log_sum,
        attn_low,
        standard_two,
        inv_two,
        mixed_low,
        up_proj,
        activated,
        standard_three,
        inv_three,
    )
    return (normed_three, saved)


def layer_backward(
    grad_out,
    params,
    saved,
    edge_feat,
    edge_src,
    edge_dst,
    halo_send,
    local_graphs,
    group_graphs,
    node_total,
):
    w_proj, w_edge, w_qkv, w_out, w_up, w_down, norm_gains, norm_shifts = params
    (
        hidden_low,
        source_b,
        gating,
        numerator,
        denominator,
        normed_one,
        standard_one,
        inv_one,
        query_rows,
        key_rows,
        value_rows,
        attn_raw,
        log_sum,
        attn_low,
        standard_two,
        inv_two,
        mixed_low,
        up_proj,
        activated,
        standard_three,
        inv_three,
    ) = saved
    row_count, model_width = grad_out.shape
    grad_three, gain_three, shift_three = normalize_back(
        grad_out, standard_three, inv_three, norm_gains[2], node_total
    )
    down_grad = grad_three.astype(jnp.bfloat16)
    grad_w_down = outer_product(activated, down_grad)
    up_grad = (times_transposed(down_grad, w_down) * silu_slope_plain(up_proj)).astype(jnp.bfloat16)
    grad_w_up = outer_product(mixed_low, up_grad)
    grad_mixed = grad_three + times_transposed(up_grad, w_up)
    grad_two, gain_two, shift_two = normalize_back(
        grad_mixed, standard_two, inv_two, norm_gains[1], node_total
    )
    out_grad = grad_two.astype(jnp.bfloat16)
    grad_w_out = outer_product(attn_low, out_grad)
    attn_grad = times_transposed(out_grad, w_out).astype(jnp.bfloat16)
    grad_query, grad_key, grad_value = attend_backward(
        query_rows, key_rows, value_rows, attn_grad, attn_raw, log_sum, local_graphs, group_graphs
    )
    qkv_grad = jnp.concatenate([grad_query, grad_key, grad_value], 1).astype(jnp.bfloat16)
    grad_w_qkv = outer_product(hidden_low, qkv_grad)
    grad_message, gain_one, shift_one = normalize_back(
        grad_mixed * silu_slope_plain(normed_one), standard_one, inv_one, norm_gains[0], node_total
    )
    shifted = denominator + GATE_EPS
    grad_numer = grad_message / shifted
    grad_denom = -grad_message * numerator / (shifted * shifted)
    numer_edge = grad_numer[edge_dst]
    grad_gate = numer_edge * source_b + grad_denom[edge_dst]
    grad_pre_edge = grad_gate * gating * (1.0 - gating)
    edge_grad = grad_pre_edge.astype(jnp.bfloat16)
    grad_w_edge = outer_product(edge_feat, edge_grad)
    grad_dest = jax.ops.segment_sum(grad_pre_edge, edge_dst, row_count)
    grad_extended = jax.ops.segment_sum(
        jnp.concatenate([numer_edge * gating, grad_pre_edge], 1),
        edge_src,
        row_count + halo_send.shape[0],
    )
    returned = return_sources(grad_extended[row_count:])
    grad_source = grad_extended[:row_count].at[halo_send].add(returned)
    proj_grad = jnp.concatenate(
        [grad_message, grad_source[:, :model_width], grad_dest, grad_source[:, model_width:]], 1
    ).astype(jnp.bfloat16)
    grad_w_proj = outer_product(hidden_low, proj_grad)
    grad_hidden = (
        grad_mixed
        + grad_two
        + times_transposed(proj_grad, w_proj)
        + times_transposed(qkv_grad, w_qkv)
    )
    weight_grads = (grad_w_proj, grad_w_edge, grad_w_qkv, grad_w_out, grad_w_up, grad_w_down)
    return (
        grad_hidden,
        weight_grads,
        jnp.stack([gain_one, gain_two, gain_three]),
        jnp.stack([shift_one, shift_two, shift_three]),
    )


def per_device(
    node_input,
    edge_feat,
    graph_ids,
    edge_src,
    edge_dst,
    halo_send,
    w_proj,
    w_edge,
    w_qkv,
    w_out,
    w_up,
    w_down,
    norm_gain,
    norm_shift,
    cotangent,
):
    group_graphs = lax.all_gather(graph_ids, "nodes", axis=0, tiled=True)
    node_total = node_input.shape[0] * lax.axis_size("nodes") * lax.axis_size("rep")
    layer_count = w_proj.shape[0]
    layer_params = [
        (
            w_proj[layer_index],
            w_edge[layer_index],
            w_qkv[layer_index],
            w_out[layer_index],
            w_up[layer_index],
            w_down[layer_index],
            norm_gain[layer_index],
            norm_shift[layer_index],
        )
        for layer_index in range(layer_count)
    ]
    hidden = node_input.astype(jnp.float32)
    saved_all = []
    for layer_index in range(layer_count):
        hidden, saved = layer_forward(
            hidden,
            layer_params[layer_index],
            edge_feat,
            edge_src,
            edge_dst,
            halo_send,
            graph_ids,
            group_graphs,
            node_total,
        )
        saved_all.append(saved)
    grad_hidden = cotangent.astype(jnp.float32)
    weight_parts = [None] * layer_count
    gain_parts = [None] * layer_count
    shift_parts = [None] * layer_count
    for layer_index in range(layer_count - 1, -1, -1):
        (
            grad_hidden,
            weight_parts[layer_index],
            gain_parts[layer_index],
            shift_parts[layer_index],
        ) = layer_backward(
            grad_hidden,
            layer_params[layer_index],
            saved_all[layer_index],
            edge_feat,
            edge_src,
            edge_dst,
            halo_send,
            graph_ids,
            group_graphs,
            node_total,
        )
    proj_local = jnp.stack([weight_parts[layer_index][0] for layer_index in range(layer_count)])
    edge_local = jnp.stack([weight_parts[layer_index][1] for layer_index in range(layer_count)])
    qkv_local = jnp.stack([weight_parts[layer_index][2] for layer_index in range(layer_count)])
    out_local = jnp.stack([weight_parts[layer_index][3] for layer_index in range(layer_count)])
    up_local = jnp.stack([weight_parts[layer_index][4] for layer_index in range(layer_count)])
    down_local = jnp.stack([weight_parts[layer_index][5] for layer_index in range(layer_count)])
    grad_proj, grad_edge, grad_qkv, grad_out, grad_up, grad_down = lax.psum(
        (proj_local, edge_local, qkv_local, out_local, up_local, down_local), ("nodes", "rep")
    )
    return (
        hidden,
        grad_hidden,
        grad_proj,
        grad_edge,
        grad_qkv,
        grad_out,
        grad_up,
        grad_down,
        jnp.stack(gain_parts),
        jnp.stack(shift_parts),
    )


def solution(mesh):
    in_specs = (
        P(("rep", "nodes"), None),
        P(("rep", "nodes"), None),
        P(("rep", "nodes")),
        P(("rep", "nodes")),
        P(("rep", "nodes")),
        P(("rep", "nodes")),
        P(),
        P(),
        P(),
        P(),
        P(),
        P(),
        P(),
        P(),
        P(("rep", "nodes"), None),
    )
    out_specs = (
        P(("rep", "nodes"), None),
        P(("rep", "nodes"), None),
        P(),
        P(),
        P(),
        P(),
        P(),
        P(),
        P(),
        P(),
    )
    N, M = mesh.shape["nodes"], mesh.shape["rep"]
    fused = N % 2 == 0 and N <= 8 and 512 % (16 * N * M) == 0
    return jax.shard_map(
        functools.partial(fused_device, N, M) if fused else per_device,
        mesh=mesh, in_specs=in_specs, out_specs=out_specs, check_vma=False,
    )
```

```python
import functools
import math

import jax
import jax.numpy as jnp
from jax import lax
from jax.experimental import pallas as pl
from jax.experimental.pallas import tpu as pltpu
from jax.sharding import PartitionSpec as P

HEADS = 8
HEAD_DIM = 32
NEG = -1e30
NORM_EPS = 1e-05
GATE_EPS = 1e-06
F32, BF16, I32 = jnp.float32, jnp.bfloat16, jnp.int32
MESH = pl.DeviceIdType.MESH
SYNCS = 7
GROUPS = (
    (2560, ("core", "y", "x", "z")),
    (4096, ("core", "y", "x", "z")),
    (2560, ("core", "y", "x", "z")),
    (2560, ("core", "y", "nodes")),
    (1024, ("rep", "nodes")),
    (512, ("nodes", "rep")),
)


def dot(left, right):
    return lax.dot_general(
        left, right, (((1,), (0,)), ((), ())), preferred_element_type=F32
    )


def dot_nt(left, right):
    return lax.dot_general(
        left, right, (((1,), (1,)), ((), ())), preferred_element_type=F32
    )


def dot_tn(left, right):
    return lax.dot_general(
        left, right, (((0,), (0,)), ((), ())), preferred_element_type=F32
    )


def split(value):
    high = value.astype(BF16)
    return high, (value - high.astype(F32)).astype(BF16)


def select_rows(onehot, value):
    high, low = split(value)
    return dot(onehot, high) + dot(onehot, low)


def sigmoid(value):
    return 1.0 / (1.0 + jnp.exp(-value))


def silu_slope(value):
    logistic = sigmoid(value)
    return logistic * (1.0 + value * (1.0 - logistic))


def col_sum(value):
    return jnp.sum(value, axis=0, keepdims=True)


def pack(first, second, third, fourth):
    halves = []
    for row in (first, second, third, fourth):
        halves += [row[:, :128], row[:, 128:]]
    return jnp.concatenate(halves, 0)


def unpack(tile):
    return [
        jnp.concatenate([tile[2 * i : 2 * i + 1], tile[2 * i + 1 : 2 * i + 2]], 1)
        for i in range(4)
    ]


def combine_pair(tiles, count):
    mean = jnp.mean(tiles[:, 0:4], 0)
    off = tiles[:, 0:4] - mean
    return jnp.concatenate([mean, jnp.sum(tiles[:, 4:8] + count * off * off, 0)], 0)


def combine_last(tiles, count):
    mean = jnp.mean(tiles[:, 0:2], 0)
    off = tiles[:, 0:2] - mean
    return jnp.concatenate(
        [
            mean,
            jnp.sum(tiles[:, 2:4], 0),
            jnp.sum(tiles[:, 4:6] + count * off * off, 0),
            jnp.sum(tiles[:, 6:8] + off * tiles[:, 2:4], 0),
        ],
        0,
    )


def combine_sum(tiles, count):
    return jnp.sum(tiles, 0)


class Refs:
    pass


def axis_sizes(N, M):
    return dict(core=2, y=M // 2, x=2, z=N // 2, rep=M, nodes=N)


def scratch_list(N, M, L, R, E):
    NZ, G, HR = N // 2, N * R, HEADS * R
    D, FF = 256, 512
    dma = lambda *shape: pltpu.SemaphoreType.DMA(shape)
    vm = lambda dtype, *shape: pltpu.VMEM(shape, dtype)
    names = dict(
        xs=vm(BF16, L, N, R, D),
        yc=vm(BF16, N, R, D),
        meta=vm(I32, N, 8, 256),
        ef=vm(BF16, E, D),
        cot=vm(BF16, R, D),
        wp=vm(BF16, L, D, 4 * D),
        we=vm(BF16, L, D, D),
        wqkv=vm(BF16, L, D, 3 * D),
        wo=vm(BF16, L, D, D),
        wu=vm(BF16, L, D, FF),
        wd=vm(BF16, L, FF, D),
        oact=vm(F32, R, D),
        gin=vm(F32, R, D),
        dce=vm(BF16, E, D),
        dproj=vm(BF16, 4, 256, D),
        xeT=vm(BF16, L, D, 256),
        st1=vm(F32, SYNCS, N, 8, 128),
        st2=vm(F32, SYNCS, M, 8, 128),
        T=vm(BF16, E, R),
        TT=vm(BF16, R, E),
        S=vm(BF16, E, 256),
        ST=vm(BF16, 256, E),
        efT=vm(BF16, D, E),
        HP=vm(BF16, 32, R),
        HN=vm(BF16, 32, R),
        A=vm(BF16, R, 64),
        bias=vm(F32, R, G),
        ce=vm(F32, L, E, D),
        xf=vm(F32, L, R, D),
        xe=vm(BF16, L, 256, D),
        gate=vm(F32, L, E, D),
        bs=vm(BF16, L, E, D),
        num=vm(F32, L, R, D),
        den=vm(F32, L, R, D),
        z0=vm(F32, L, R, D),
        z1=vm(F32, L, R, D),
        z2=vm(F32, L, R, D),
        kk=vm(BF16, L, G, D),
        vv=vm(BF16, L, G, D),
        kT=vm(BF16, D, G),
        vT=vm(BF16, D, G),
        od=vm(F32, NZ // 2, R, D),
        md=vm(F32, NZ // 2, R, D),
        ld=vm(F32, NZ // 2, R, D),
        rb=vm(F32, L, NZ // 2, R, D),
        dob=vm(F32, R, D),
        dq=vm(F32, R, D),
        pst=vm(BF16, L, HR, G),
        oraw=vm(F32, L, R, D),
        ob=vm(BF16, L, R, D),
        mb=vm(BF16, L, R, D),
        u=vm(F32, L, R, FF),
        g=vm(BF16, L, R, FF),
        iv=vm(F32, L, 8, D),
        dmix=vm(F32, R, D),
        dxo=vm(F32, R, D),
        qm=vm(BF16, L, HR, D),
        qmT=vm(BF16, D, HR),
        dom=vm(BF16, HR, D),
        domT=vm(BF16, D, HR),
        dss=vm(BF16, HR, G),
        gkv=vm(F32, 2 * D, D),
        dxs=vm(BF16, L, NZ, 2, R, D),
        rs1=vm(BF16, L, NZ, R, D),
        cs=vm(BF16, L, NZ, R, D),
        rs2=vm(BF16, L, NZ, R, D),
        hs=vm(BF16, L, 2, 32, D),
        hr=vm(BF16, L, 2, 32, D),
    )
    sizes = axis_sizes(N, M)
    for g, (rows, stages) in enumerate(GROUPS):
        names[f"gs{g}"] = vm(BF16, rows, 128)
        names[f"go{g}"] = vm(BF16, rows, 128)
        left = rows
        for k, axis in enumerate(stages):
            left //= sizes[axis]
            names[f"ga{g}_{k}"] = vm(BF16, sizes[axis] - 1, left, 128)
            if k < len(stages) - 1:
                names[f"gh{g}_{k}"] = vm(BF16, left, 128)
    names.update(
        load=dma(10),
        store=dma(2),
        meta_s=dma(1),
        meta_r=dma(1),
        st1_s=dma(SYNCS),
        st1_r=dma(SYNCS),
        st2_s=dma(SYNCS),
        st2_r=dma(SYNCS),
        agc_s=dma(L, NZ),
        agc_r=dma(L, NZ),
        agp_s=dma(L, NZ),
        agp_r=dma(L, NZ),
        rsp_s=dma(L, NZ),
        rsp_r=dma(L, NZ),
        rsc_s=dma(L, NZ),
        rsc_r=dma(L, NZ),
        hal_s=dma(L, 2),
        hal_r=dma(L, 2),
        ar_s=dma(len(GROUPS), 8),
        ar_r=dma(len(GROUPS), 8),
        ar_l=dma(len(GROUPS)),
    )
    return names


IN_NAMES = (
    "x_in", "ids", "edge_src", "edge_dst", "halo", "ef_h", "wp_h", "we_h", "wqkv_h", "wo_h", "wu_h", "wd_h",
    "gain", "shift", "cot_h",
)
OUT_NAMES = ("out_act", "grad_in", *(f"gout{g}" for g in range(len(GROUPS))), "ggain", "gshift")


def kernel(N, M, L, names, *args):
    r_ = Refs()
    for name, ref in zip(IN_NAMES + OUT_NAMES + tuple(names), args, strict=True):
        setattr(r_, name, ref)
    R, D = r_.x_in.shape
    E = r_.ef.shape[0]
    NZ, NB, G, W = N // 2, N // 4, N * R, 4 * R
    total = float(N * M * R)
    scale = HEAD_DIM ** -0.5
    me = lax.axis_index("nodes")
    rep = lax.axis_index("rep")
    z = me // 2
    par = me % 2
    partner = 2 * z + (1 - par)
    prev = (me + N - 1) % N
    nxt = (me + 1) % N
    zh, zl = z // 2, z % 2
    z_to = lambda t: 2 * ((zh + t // 2) % NB) + (zl + t % 2) % 2
    z_from = lambda t: 2 * ((zh + NB - t // 2) % NB) + (zl + t % 2) % 2
    drains = []

    def remote(src, dst, s_sem, r_sem, **where):
        return pltpu.make_async_remote_copy(
            src_ref=src, dst_ref=dst, send_sem=s_sem, recv_sem=r_sem,
            device_id=where, device_id_type=MESH,
        )

    def send(src, dst, s_sem, r_sem, **where):
        remote(src, dst, s_sem, r_sem, **where).start()

    def arrive(dst, r_sem):
        remote(dst, dst, r_sem, r_sem, nodes=partner).wait_recv()

    def sent(src, s_sem):
        drains.append((src, s_sem))

    loads = [
        pltpu.make_async_copy(getattr(r_, f"{name}_h"), getattr(r_, name), r_.load.at[i])
        for i, name in enumerate(("ef", "we", "wqkv", "wp", "wo", "wu", "wd", "cot"))
    ]
    own_rows = pltpu.make_async_copy(r_.x_in, r_.xs.at[0, me], r_.load.at[8])
    own_rows.start()
    for load in loads:
        load.start()

    barrier = pltpu.get_barrier_semaphore()
    for d in range(1, N):
        pl.semaphore_signal(barrier, inc=1, device_id={"nodes": (me + d) % N}, device_id_type=MESH)
    for d in range(1, M):
        pl.semaphore_signal(barrier, inc=1, device_id={"rep": (rep + d) % M}, device_id_type=MESH)
    pl.semaphore_wait(barrier, N + M - 2)

    def gather_start(buf, l):
        send(buf.at[me], buf.at[me], r_.agp_s.at[l, 0], r_.agp_r.at[l, 0], nodes=partner)
        sent(buf.at[me], r_.agp_s.at[l, 0])
        for t in range(1, NZ):
            send(buf.at[me], buf.at[me], r_.agc_s.at[l, t], r_.agc_r.at[l, t], nodes=2 * z_to(t) + par)
            sent(buf.at[me], r_.agc_s.at[l, t])

    def gather_pass(buf, l, t):
        c = 2 * z_from(t) + par
        arrive(buf.at[c], r_.agc_r.at[l, t])
        send(buf.at[c], buf.at[c], r_.agp_s.at[l, t], r_.agp_r.at[l, t], nodes=partner)

    def gather_take(buf, l, t):
        arrive(buf.at[2 * z_from(t) + 1 - par], r_.agp_r.at[l, t])

    def gather_drain(buf, l):
        for t in range(1, NZ):
            sent(buf.at[0], r_.agp_s.at[l, t])

    def sync_start(k, tile):
        r_.st1[k, me] = tile
        for d in range(1, N):
            send(r_.st1.at[k, me], r_.st1.at[k, me], r_.st1_s.at[k], r_.st1_r.at[k], nodes=(me + d) % N)
        sent(r_.st1.at[k, 0 : N - 1], r_.st1_s.at[k])

    def sync_finish(k, combine):
        arrive(r_.st1.at[k, 0 : N - 1], r_.st1_r.at[k])
        r_.st2[k, rep] = combine(r_.st1[k], float(R))
        for d in range(1, M):
            send(r_.st2.at[k, rep], r_.st2.at[k, rep], r_.st2_s.at[k], r_.st2_r.at[k], rep=(rep + d) % M)
        sent(r_.st2.at[k, 0 : M - 1], r_.st2_s.at[k])
        arrive(r_.st2.at[k, 0 : M - 1], r_.st2_r.at[k])
        return unpack(combine(r_.st2[k], float(R * N)))

    sizes = axis_sizes(N, M)
    core, row = rep % 2, rep // 2
    places = dict(
        core=(core, lambda t: dict(rep=2 * row + t)),
        y=(row, lambda t: dict(rep=2 * t + core)),
        x=(par, lambda t: dict(nodes=2 * z + t)),
        z=(z, lambda t: dict(nodes=2 * t + par)),
        rep=(rep, lambda t: dict(rep=t)),
        nodes=(me, lambda t: dict(nodes=t)),
    )

    def reduce_step(g, step):
        rows, stages = GROUPS[g]
        K = len(stages)
        gs, out = getattr(r_, f"gs{g}"), getattr(r_, f"go{g}")
        count, offset = [rows], [0]
        for axis in stages:
            count.append(count[-1] // sizes[axis])
            offset.append(offset[-1] + places[axis][0] * count[-1])
        take = lambda start, size: pl.ds(pl.multiple_of(start, 16), size)
        if 1 <= step <= K:
            k = step - 1
            got = getattr(r_, f"ga{g}_{k}")
            arrive(got, r_.ar_r.at[g, k])
            held = gs if k == 0 else getattr(r_, f"gh{g}_{k - 1}")
            index = places[stages[k]][0]
            acc = held[take(index * count[k + 1], count[k + 1])].astype(F32)
            for slot in range(sizes[stages[k]] - 1):
                acc = acc + got[slot].astype(F32)
            if step < K:
                getattr(r_, f"gh{g}_{k}")[...] = acc.astype(BF16)
            else:
                out[take(offset[K], count[K])] = acc.astype(BF16)
        elif step > K:
            k = 2 * K - step
            arrive(out.at[0 : (sizes[stages[k]] - 1) * count[k + 1]], r_.ar_r.at[g, step - 1])
        if step < K:
            held = gs if step == 0 else getattr(r_, f"gh{g}_{step - 1}")
            index, device = places[stages[step]]
            size = sizes[stages[step]]
            for d in range(1, size):
                to = (index + d) % size
                send(held.at[take(to * count[step + 1], count[step + 1])], getattr(r_, f"ga{g}_{step}").at[d - 1],
                     r_.ar_s.at[g, step], r_.ar_r.at[g, step], **device(to))
        elif step < 2 * K:
            k = 2 * K - 1 - step
            index, device = places[stages[k]]
            size = sizes[stages[k]]
            here = out.at[take(offset[k + 1], count[k + 1])]
            for d in range(1, size):
                send(here, here, r_.ar_s.at[g, step], r_.ar_r.at[g, step], **device((index + d) % size))
        else:
            pltpu.make_async_copy(out, getattr(r_, f"gout{g}"), r_.ar_l.at[g]).start()

    def reduce_drain(g):
        rows, stages = GROUPS[g]
        K, left = len(stages), rows
        out = getattr(r_, f"go{g}")
        for k, axis in enumerate(stages):
            left //= sizes[axis]
            for step in (k, 2 * K - 1 - k):
                sent(out.at[0 : (sizes[axis] - 1) * left], r_.ar_s.at[g, step])
        pltpu.make_async_copy(out, getattr(r_, f"gout{g}"), r_.ar_l.at[g]).wait()

    def put(buf, at, value):
        rows = value.shape[0]
        for c in range(value.shape[1] // 128):
            buf[at : at + rows] = value[:, 128 * c : 128 * (c + 1)].astype(BF16)
            at += rows
        return at

    lane_head = lax.broadcasted_iota(I32, (R, D), 1) // HEAD_DIM

    r_.meta[me] = jnp.full((8, 256), -1, I32)
    r_.meta[me, 0:1, 0:R] = r_.ids[...].reshape(1, R)
    r_.meta[me, 1:2, 0:48] = r_.halo[...].reshape(1, 48)
    for d in range(1, N):
        send(r_.meta.at[me], r_.meta.at[me], r_.meta_s.at[0], r_.meta_r.at[0], nodes=(me + d) % N)
    sent(r_.meta.at[0 : N - 1], r_.meta_s.at[0])
    own_rows.wait()
    gather_start(r_.xs.at[0], 0)

    src_row = r_.edge_src[...].reshape(1, E)
    src_row = jnp.where(src_row < R + 24, src_row, src_row + 8)
    dst_row = r_.edge_dst[...].reshape(1, E)
    src_col = jnp.broadcast_to(src_row, (128, E)).T[:, 0:1]
    dst_col = jnp.broadcast_to(dst_row, (128, E)).T[:, 0:1]
    as_mask = lambda cond: cond.astype(F32).astype(BF16)
    r_.T[...] = as_mask(dst_col == lax.broadcasted_iota(I32, (E, R), 1))
    r_.TT[...] = as_mask(dst_row == lax.broadcasted_iota(I32, (R, E), 0))
    r_.S[...] = as_mask(src_col == lax.broadcasted_iota(I32, (E, 256), 1))
    r_.ST[...] = as_mask(src_row == lax.broadcasted_iota(I32, (256, E), 0))
    loads[0].wait()
    r_.efT[...] = r_.ef[...].T
    loads[1].wait()
    for l in range(L):
        r_.ce[l] = dot(r_.ef[...], r_.we[l])
    r_.xf[0] = r_.xs[0, me].astype(F32)
    for load in loads[2:]:
        load.wait()

    arrive(r_.meta.at[0 : N - 1], r_.meta_r.at[0])
    id_col = jnp.broadcast_to(r_.meta[me][0:1, 0:R], (128, R)).T[:, 0:1]
    id_row = jnp.concatenate([r_.meta[j][0:1, 0:R] for j in range(N)], 1)
    r_.bias[...] = jnp.where(id_col == id_row, 0.0, NEG)

    def halo_onehot(device, start):
        row = jnp.broadcast_to(r_.meta[device][1:2, 0:128], (128, 128)).T[start : start + 24, 0:1]
        hot = (row == lax.broadcasted_iota(I32, (24, R), 1)).astype(F32)
        return jnp.concatenate([hot, jnp.zeros((8, R), F32)], 0).astype(BF16)

    r_.HP[...] = halo_onehot(prev, 24)
    r_.HN[...] = halo_onehot(nxt, 0)
    r_.A[...] = as_mask(r_.meta[me][1:2, 0:64] == lax.broadcasted_iota(I32, (R, 64), 0))

    def prepare_queries(l):
        q = dot(r_.xs[l, me], r_.wqkv[l, :, :D]).astype(BF16).astype(F32)
        for h in range(HEADS):
            r_.qm[l, h * R : (h + 1) * R] = jnp.where(lane_head == h, q, 0.0).astype(BF16)

    factor_exp = scale * math.log2(math.e)
    CH = 2 * R

    def attention_block(l, i, middle):
        half = (zh + NB - i) % NB
        rows = pl.ds(pl.multiple_of(half * W, 128), W)
        x = r_.xs[l, pl.ds(4 * half, 4)].reshape(W, D)
        key = dot(x, r_.wqkv[l, :, D : 2 * D]).astype(BF16)
        value = dot(x, r_.wqkv[l, :, 2 * D :]).astype(BF16)
        r_.kk[l, rows] = key
        r_.vv[l, rows] = value
        r_.kT[:, rows] = key.T
        for c in range(HEADS // 2):
            both = slice(c * CH, (c + 1) * CH)
            scores = dot(r_.qm[l, both], r_.kT[:, rows])
            for k in range(2):
                h = 2 * c + k
                lanes = slice(h * HEAD_DIM, (h + 1) * HEAD_DIM)
                s = scores[k * R : (k + 1) * R] + r_.bias[:, rows]
                top = jnp.max(s, 1, keepdims=True)
                e = jnp.exp2((s - top) * factor_exp)
                r_.md[i, :, lanes] = jnp.broadcast_to(top, (R, HEAD_DIM))
                r_.ld[i, :, lanes] = jnp.broadcast_to(jnp.sum(e, 1, keepdims=True), (R, HEAD_DIM))
                r_.pst[l, h * R : (h + 1) * R, rows] = e.astype(BF16)
            o = dot(r_.pst[l, both, rows], r_.vv[l, rows])
            for k in range(2):
                h = 2 * c + k
                lanes = slice(h * HEAD_DIM, (h + 1) * HEAD_DIM)
                r_.od[i, :, lanes] = o[k * R : (k + 1) * R, lanes]
            middle(c)

    def attention_end(l):
        top = r_.md[0]
        for i in range(1, NB):
            top = jnp.maximum(top, r_.md[i])
        factors = [jnp.exp2((r_.md[i] - top) * factor_exp) for i in range(NB)]
        inv = 1.0 / sum(factors[i] * r_.ld[i] for i in range(NB))
        o = jnp.zeros((R, D), F32)
        for i in range(NB):
            r_.rb[l, i] = factors[i] * inv
            o = o + factors[i] * inv * r_.od[i]
        r_.oraw[l] = o
        ob = o.astype(BF16)
        r_.ob[l] = ob
        t1 = r_.xf[l] + dot(ob, r_.wo[l])
        r_.z1[l] = t1
        mean1 = col_sum(t1) / R
        return mean1, col_sum((t1 - mean1) * (t1 - mean1))

    def convolution(l):
        xs = r_.xs
        xb = xs[l, me]
        r_.xe[l, 0:R] = xb
        r_.xe[l, R : R + 32] = dot(r_.HP[...], xs[l, prev]).astype(BF16)
        r_.xe[l, R + 32 : R + 64] = dot(r_.HN[...], xs[l, nxt]).astype(BF16)
        xe = r_.xe[l]
        tab_b = dot(xe, r_.wp[l, :, D : 2 * D]).astype(BF16)
        tab_e = dot(xe, r_.wp[l, :, 3 * D :]).astype(BF16)
        pa = dot(xb, r_.wp[l, :, 0:D])
        pd = dot(xb, r_.wp[l, :, 2 * D : 3 * D])
        bs = dot(r_.S[...], tab_b)
        r_.bs[l] = bs.astype(BF16)
        gate = sigmoid(select_rows(r_.T[...], pd) + dot(r_.S[...], tab_e) + r_.ce[l])
        r_.gate[l] = gate
        num = select_rows(r_.TT[...], gate * bs)
        den = select_rows(r_.TT[...], gate)
        r_.num[l] = num
        r_.den[l] = den
        msg = pa + num / (den + GATE_EPS)
        r_.z0[l] = msg
        mean0 = col_sum(msg) / R
        return mean0, col_sum((msg - mean0) * (msg - mean0))

    def layer_forward(l, buf, ready):
        gather_pass(buf, l, 1)
        prepare_queries(l)
        gather_take(buf, l, 0)
        gather_take(buf, l, 1)
        ready([partner, 2 * z_from(1) + par, 2 * z_from(1) + 1 - par])

        def middle(c):
            if c < NZ - 2:
                gather_pass(buf, l, c + 2)

        attention_block(l, 0, middle)
        for t in range(2, NZ):
            gather_take(buf, l, t)
        gather_drain(buf, l)
        ready([2 * z_from(t) + p for t in range(2, NZ) for p in range(2)])
        mean0, sq0 = convolution(l)
        for i in range(1, NB):
            attention_block(l, i, lambda c: None)
        mean1, sq1 = attention_end(l)
        sync_start(2 * l, pack(mean0, mean1, sq0, sq1))

    def layer_forward_rest(l):
        mean0, mean1, sq0, sq1 = sync_finish(2 * l, combine_pair)
        inv0 = lax.rsqrt(sq0 / total + NORM_EPS)
        inv1 = lax.rsqrt(sq1 / total + NORM_EPS)
        r_.iv[l, 0:1] = inv0
        r_.iv[l, 1:2] = inv1
        z0 = (r_.z0[l] - mean0) * inv0
        z1 = (r_.z1[l] - mean1) * inv1
        r_.z0[l] = z0
        r_.z1[l] = z1
        n0 = z0 * r_.gain[0, l : l + 1] + r_.shift[0, l : l + 1]
        mix = r_.xf[l] + n0 * sigmoid(n0) + z1 * r_.gain[1, l : l + 1] + r_.shift[1, l : l + 1]
        mb = mix.astype(BF16)
        r_.mb[l] = mb
        u = dot(mb, r_.wu[l])
        r_.u[l] = u
        g = (u * sigmoid(u)).astype(BF16)
        r_.g[l] = g
        return mix + dot(g, r_.wd[l])

    zero_row = jnp.zeros((1, D), F32)
    layer_forward(0, r_.xs.at[0], lambda js: None)
    for l in range(L):
        y = layer_forward_rest(l)
        r_.z2[l] = y
        mean = col_sum(y) / R
        cent = y - mean
        sq = col_sum(cent * cent)
        gain, shift = r_.gain[2, l : l + 1], r_.shift[2, l : l + 1]
        k = 2 * l + 1
        if l < L - 1:
            r_.yc[me] = cent.astype(BF16)
            sync_start(k, pack(mean, zero_row, sq, zero_row))
            gather_start(r_.yc, l + 1)
            tot_mean, _, tot_sq, _ = sync_finish(k, combine_last)
            inv2 = lax.rsqrt(tot_sq / total + NORM_EPS)
            r_.iv[l, 2:3] = inv2
            z2 = (r_.z2[l] - tot_mean) * inv2
            r_.z2[l] = z2
            r_.xf[l + 1] = z2 * gain + shift
            r_.xs[l + 1, me] = r_.xf[l + 1].astype(BF16)
            factor = inv2 * gain

            def ready(js, l=l, k=k, factor=factor, shift=shift, tot_mean=tot_mean):
                for j in js:
                    tile = r_.st1[k, j]
                    mean_j = jnp.concatenate([tile[0:1], tile[1:2]], 1)
                    moved = (r_.yc[j].astype(F32) + (mean_j - tot_mean)) * factor + shift
                    r_.xs[l + 1, j] = moved.astype(BF16)

            layer_forward(l + 1, r_.yc, ready)
        else:
            dy = r_.cot[...].astype(F32)
            sync_start(k, pack(mean, col_sum(dy), sq, col_sum(dy * cent)))
            for j in range(L):
                r_.xeT[j] = r_.xe[j].T
            tot_mean, dy_sum, tot_sq, dy_cent = sync_finish(k, combine_last)
            inv2 = lax.rsqrt(tot_sq / total + NORM_EPS)
            r_.iv[l, 2:3] = inv2
            z2 = (r_.z2[l] - tot_mean) * inv2
            r_.z2[l] = z2
            r_.oact[...] = z2 * gain + shift
            pltpu.make_async_copy(r_.oact, r_.out_act, r_.store.at[0]).start()
            sums = (dy_sum, dy_cent * inv2)

    k_back = {1: 4, 0: 6}

    def back_feed_forward(l, dy, sums):
        s2, g2 = sums
        r_.gshift[2, l : l + 1] = s2
        r_.ggain[2, l : l + 1] = g2
        d3 = r_.gain[2, l : l + 1] * r_.iv[l, 2:3] * (dy - s2 / total - r_.z2[l] * (g2 / total))
        db = d3.astype(BF16)
        dub = (dot_nt(db, r_.wd[l]) * silu_slope(r_.u[l])).astype(BF16)
        dmix = d3 + dot_nt(dub, r_.wu[l])
        r_.dmix[...] = dmix
        n0 = r_.z0[l] * r_.gain[0, l : l + 1] + r_.shift[0, l : l + 1]
        gy0 = dmix * silu_slope(n0)
        sync_start(k_back[l], pack(col_sum(dmix), col_sum(dmix * r_.z1[l]), col_sum(gy0), col_sum(gy0 * r_.z0[l])))
        early = r_.gs0 if l == L - 1 else r_.gs2
        at = put(early, 512, dot_tn(r_.mb[l], dub))
        put(early, at, dot_tn(r_.g[l], db))
        r_.qmT[...] = r_.qm[l].T
        r_.vT[...] = r_.vv[l].T

    def back_norms(l):
        s1, g1, s0, g0 = sync_finish(k_back[l], combine_sum)
        r_.gshift[1, l : l + 1] = s1
        r_.ggain[1, l : l + 1] = g1
        r_.gshift[0, l : l + 1] = s0
        r_.ggain[0, l : l + 1] = g0
        dmix = r_.dmix[...]
        d2 = r_.gain[1, l : l + 1] * r_.iv[l, 1:2] * (dmix - s1 / total - r_.z1[l] * (g1 / total))
        dab = d2.astype(BF16)
        r_.dxo[...] = dmix + d2
        put(r_.gs0 if l == L - 1 else r_.gs2, 0, dot_tn(r_.ob[l], dab))
        dob = dot_nt(dab, r_.wo[l]).astype(BF16).astype(F32)
        r_.dob[...] = dob

    def back_attention(l, between):
        r_.gkv[...] = jnp.zeros((2 * D, D), F32)
        r_.dq[...] = jnp.zeros((R, D), F32)

        def block(i, carry):
            t1 = (i + 1) % NB
            half = (zh + t1) % NB
            rows = pl.ds(pl.multiple_of(half * W, 128), W)
            dos = r_.dob[...] * r_.rb[l, (NB - t1) % NB]
            prod = dos * r_.oraw[l]
            for h in range(HEADS):
                r_.dom[h * R : (h + 1) * R] = jnp.where(lane_head == h, dos, 0.0).astype(BF16)
            r_.domT[...] = r_.dom[...].T
            for c in range(HEADS // 2):
                both = slice(c * CH, (c + 1) * CH)
                dp = dot(r_.dom[both], r_.vT[:, rows])
                for k in range(2):
                    h = 2 * c + k
                    mine = slice(h * R, (h + 1) * R)
                    delta = jnp.sum(jnp.where(lane_head == h, prod, 0.0), 1, keepdims=True)
                    ds = r_.pst[l, mine, rows].astype(F32) * (dp[k * R : (k + 1) * R] - delta)
                    r_.dss[mine, rows] = ds.astype(BF16)
                part = dot(r_.dss[both, rows], r_.kk[l, rows])
                for k in range(2):
                    h = 2 * c + k
                    lanes = slice(h * HEAD_DIM, (h + 1) * HEAD_DIM)
                    r_.dq[:, lanes] += part[k * R : (k + 1) * R, lanes]
                between(i, c)
            dk = (dot(r_.qmT[...], r_.dss[:, rows]) * scale).astype(BF16)
            dv = dot(r_.domT[...], r_.pst[l, :, rows]).astype(BF16)
            dkv = jnp.concatenate([dk, dv], 0)
            dx = dot(r_.wqkv[l, :, D:], dkv).T
            r_.dxs[l, pl.ds(2 * half, 2)] = dx.astype(BF16).reshape(2, 2, R, D)
            for low in range(2):
                zb = 2 * half + low
                send(r_.dxs.at[l, zb, 1 - par], r_.rs1.at[l, zb],
                     r_.rsp_s.at[l, 2 * i + low], r_.rsp_r.at[l, 2 * i + low], nodes=partner)
            r_.gkv[...] += dot(dkv, r_.xs[l, pl.ds(4 * half, 4)].reshape(W, D))
            between(i, HEADS // 2)
            return carry

        lax.fori_loop(0, NB, block, 0)
        for i in range(NZ):
            sent(r_.dxs.at[l, i, 0], r_.rsp_s.at[l, i])

    def pass_on(l, i, t):
        zb = z_to(t)
        arrive(r_.rs1.at[l, zb], r_.rsp_r.at[l, 2 * i + zb % 2])
        both = r_.dxs[l, zb, par].astype(F32) + r_.rs1[l, zb].astype(F32)
        r_.cs[l, zb] = both.astype(BF16)
        send(r_.cs.at[l, zb], r_.rs2.at[l, z], r_.rsc_s.at[l, t], r_.rsc_r.at[l, t], nodes=2 * zb + par)

    def back_queries(l):
        dqb = (r_.dq[...] * scale).astype(BF16)
        r_.dxo[...] += dot_nt(dqb, r_.wqkv[l, :, 0:D])
        return dqb

    def back_convolution(l):
        s0, g0 = r_.gshift[0, l : l + 1], r_.ggain[0, l : l + 1]
        inv_den = 1.0 / (r_.den[l] + GATE_EPS)
        n0 = r_.z0[l] * r_.gain[0, l : l + 1] + r_.shift[0, l : l + 1]
        gy0 = r_.dmix[...] * silu_slope(n0)
        dm = r_.gain[0, l : l + 1] * r_.iv[l, 0:1] * (gy0 - s0 / total - r_.z0[l] * (g0 / total))
        dnum = dm * inv_den
        dden = -dnum * r_.num[l] * inv_den
        dnum_e = select_rows(r_.T[...], dnum)
        dden_e = select_rows(r_.T[...], dden)
        gate = r_.gate[l]
        dgp = (dnum_e * r_.bs[l].astype(F32) + dden_e) * gate * (1.0 - gate)
        r_.dce[...] = dgp.astype(BF16)
        dpb = select_rows(r_.ST[...], dnum_e * gate).astype(BF16)
        dpe = select_rows(r_.ST[...], dgp).astype(BF16)
        dpd = select_rows(r_.TT[...], dgp).astype(BF16)
        dmb = dm.astype(BF16)
        dxe = dot_nt(dpb, r_.wp[l, :, D : 2 * D]) + dot_nt(dpe, r_.wp[l, :, 3 * D :])
        r_.hs[l, 0] = dxe[R : R + 32].astype(BF16)
        r_.hs[l, 1] = dxe[R + 32 : R + 64].astype(BF16)
        send(r_.hs.at[l, 0], r_.hr.at[l, 1], r_.hal_s.at[l, 0], r_.hal_r.at[l, 0], nodes=prev)
        send(r_.hs.at[l, 1], r_.hr.at[l, 0], r_.hal_s.at[l, 1], r_.hal_r.at[l, 1], nodes=nxt)
        sent(r_.hs.at[l, 0], r_.hal_s.at[l, 0])
        sent(r_.hs.at[l, 1], r_.hal_s.at[l, 1])
        r_.dxo[...] += (
            dxe[0:R]
            + dot_nt(dmb, r_.wp[l, :, 0:D])
            + dot_nt(dpd, r_.wp[l, :, 2 * D : 3 * D])
        )
        r_.dproj[0, 0:R] = dmb
        r_.dproj[1] = dpb
        r_.dproj[2, 0:R] = dpd
        r_.dproj[3] = dpe

    def conv_weight_grads(l, buf, at):
        for c in range(4):
            width = R if c % 2 == 0 else 256
            at = put(buf, at, dot(r_.xeT[l, :, 0:width], r_.dproj[c, 0:width]))
        put(buf, at, dot(r_.efT[...], r_.dce[...]))

    def back_input(l):
        dx = r_.dxo[...]
        arrive(r_.rs1.at[l, z], r_.rsp_r.at[l, 2 * (NB - 1) + zl])
        dx = dx + r_.dxs[l, z, par].astype(F32) + r_.rs1[l, z].astype(F32)
        for t in range(1, NZ):
            c = z_from(t)
            arrive(r_.rs2.at[l, c], r_.rsc_r.at[l, t])
            sent(r_.cs.at[l, 0], r_.rsc_s.at[l, t])
            dx = dx + r_.rs2[l, c].astype(F32)
        arrive(r_.hr.at[l, 0], r_.hal_r.at[l, 1])
        arrive(r_.hr.at[l, 1], r_.hal_r.at[l, 0])
        back = jnp.concatenate(
            [r_.hr[l, 0].astype(F32)[0:24], r_.hr[l, 1].astype(F32)[0:24], jnp.zeros((16, D), F32)], 0
        )
        return dx + dot(r_.A[...], back.astype(BF16))

    back_feed_forward(1, r_.cot[...].astype(F32), sums)
    back_norms(1)
    reduce_step(0, 0)

    def when(condition, *acts):
        @pl.when(condition)
        def _():
            for act in acts:
                act()

    step = lambda g, k: (lambda: reduce_step(g, k))
    home = lambda l, i, t: (lambda: pass_on(l, i, t))

    def between_1(i, c):
        if c == 0:
            when(i == 1, step(0, 2), home(1, 0, 2), home(1, 0, 3))
        if c == 2:
            when(i == 0, step(0, 1))
            when(i == 1, step(0, 3))

    back_attention(1, between_1)
    back_convolution(1)
    pass_on(1, NB - 1, 1)
    reduce_step(0, 4)
    dqb = back_queries(1)
    dx = back_input(1)
    r_.gin[...] = dx
    sync_start(5, pack(col_sum(dx), col_sum(dx * r_.z2[0]), zero_row, zero_row))
    at = put(r_.gs1, 0, dot(r_.xeT[1, :, 0:R], dqb))
    at = put(r_.gs1, at, r_.gkv[...].T)
    conv_weight_grads(1, r_.gs1, at)
    s2, g2, _, _ = sync_finish(5, combine_sum)
    reduce_step(1, 0)

    back_feed_forward(0, r_.gin[...], (s2, g2))
    back_norms(0)
    reduce_step(1, 1)
    reduce_step(2, 0)
    reduce_step(0, 5)
    back_convolution(0)
    reduce_step(2, 1)
    reduce_step(0, 6)
    conv_weight_grads(0, r_.gs3, 0)
    reduce_step(3, 0)
    reduce_step(1, 2)

    def between_0(i, c):
        if c == 0:
            when(i == 0, step(0, 7), step(2, 2))
            when(i == 1, home(0, 0, 2), home(0, 0, 3), step(2, 4))
        if c == 1:
            when(i == 0, step(1, 3))
            when(i == 1, step(1, 5))
        if c == 2:
            when(i == 0, step(3, 1))
            when(i == 1, step(3, 2))
        if c == 3:
            when(i == 0, step(2, 3))
            when(i == 1, step(2, 5))
        if c == 4:
            when(i == 0, step(1, 4))

    back_attention(0, between_0)
    at = put(r_.gs4, 512, r_.gkv[0:D, :].T)
    put(r_.gs5, 0, r_.gkv[D:, :].T)
    reduce_step(5, 0)
    dqb = back_queries(0)
    put(r_.gs4, 0, dot(r_.xeT[0, :, 0:R], dqb))
    reduce_step(4, 0)
    reduce_step(3, 3)
    pass_on(0, NB - 1, 1)
    reduce_step(1, 6)
    r_.gin[...] = back_input(0)
    pltpu.make_async_copy(r_.gin, r_.grad_in, r_.store.at[1]).start()
    reduce_step(5, 1)
    reduce_step(4, 1)
    reduce_step(3, 4)
    reduce_step(2, 6)
    reduce_step(1, 7)
    reduce_step(5, 2)
    reduce_step(4, 2)
    reduce_step(3, 5)
    reduce_step(2, 7)
    reduce_step(0, 8)
    reduce_step(1, 8)
    reduce_step(5, 3)
    reduce_step(4, 3)
    reduce_step(3, 6)
    reduce_step(2, 8)
    reduce_step(5, 4)
    reduce_step(4, 4)
    for g in range(len(GROUPS)):
        reduce_drain(g)
    pltpu.make_async_copy(r_.oact, r_.out_act, r_.store.at[0]).wait()
    pltpu.make_async_copy(r_.gin, r_.grad_in, r_.store.at[1]).wait()
    for src, s_sem in drains:
        remote(src, src, s_sem, s_sem, nodes=partner).wait_send()


def finish_kernel(act_h, gin_h, *refs):
    n = len(GROUPS)
    held, (ggain_h, gshift_h), refs = refs[:n], refs[n : n + 2], refs[n + 2 :]
    act_o, gin_o, proj_o, edge_o, qkv_o, out_o, up_o, down_o, ggain_o, gshift_o = refs[:10]
    summed, refs = refs[10 : 10 + n], refs[10 + n :]
    act, gin, proj, edge, qkv, out, up, down, in_sem, out_sem = refs
    loads = [
        pltpu.make_async_copy(src, dst, in_sem.at[i])
        for i, (src, dst) in enumerate(zip(held + (act_h, gin_h), summed + (act, gin), strict=True))
    ]
    for i in (1, 0, 2, 3, n, n + 1, 4, 5):
        loads[i].start()
    ggain_o[...] = ggain_h[...]
    gshift_o[...] = gshift_h[...]
    stores = []

    def store(src, dst):
        copy = pltpu.make_async_copy(src, dst, out_sem.at[len(stores)])
        copy.start()
        stores.append(copy)

    def widen(dst, l, g, at, first=0, last=None):
        rows = dst.shape[1]
        for c in range(first, dst.shape[2] // 128 if last is None else last):
            dst[l, :, 128 * c : 128 * (c + 1)] = summed[g][at : at + rows].astype(F32)
            at += rows
        return at

    loads[1].wait()
    at = widen(qkv, 1, 1, 0)
    store(qkv.at[1], qkv_o.at[1])
    at = widen(proj, 1, 1, at)
    store(proj.at[1], proj_o.at[1])
    widen(edge, 1, 1, at)
    store(edge.at[1], edge_o.at[1])
    for l, g in ((1, 0), (0, 2)):
        loads[g].wait()
        at = widen(out, l, g, 0)
        store(out.at[l], out_o.at[l])
        at = widen(up, l, g, at)
        store(up.at[l], up_o.at[l])
        widen(down, l, g, at)
        store(down.at[l], down_o.at[l])
    loads[3].wait()
    at = widen(proj, 0, 3, 0)
    store(proj.at[0], proj_o.at[0])
    widen(edge, 0, 3, at)
    store(edge.at[0], edge_o.at[0])
    loads[n].wait()
    store(act, act_o)
    loads[n + 1].wait()
    store(gin, gin_o)
    loads[4].wait()
    widen(qkv, 0, 4, 0, 0, 4)
    loads[5].wait()
    widen(qkv, 0, 5, 0, 4, 6)
    store(qkv.at[0], qkv_o.at[0])
    for copy in stores:
        copy.wait()


def fused_device(
    N, M, node_input, edge_feat, graph_ids, edge_src, edge_dst, halo_send, w_proj, w_edge, w_qkv,
    w_out, w_up, w_down, norm_gain, norm_shift, cotangent,
):
    R, D = node_input.shape
    E = edge_feat.shape[0]
    L = w_proj.shape[0]
    names = scratch_list(N, M, L, R, E)
    vmem = pl.BlockSpec(memory_space=pltpu.VMEM)
    hbm = pl.BlockSpec(memory_space=pltpu.HBM)
    shape = jax.ShapeDtypeStruct
    rows = shape((R, D), F32)
    norm = shape((3, L, D), F32)
    groups = [shape((count, 128), BF16) for count, _ in GROUPS]
    outs = pl.pallas_call(
        functools.partial(kernel, N, M, L, tuple(names)),
        out_shape=[rows, rows, *groups, norm, norm],
        in_specs=[hbm] + [vmem] * 4 + [hbm] * 7 + [vmem] * 2 + [hbm],
        out_specs=[hbm] * (2 + len(GROUPS)) + [vmem] * 2,
        scratch_shapes=list(names.values()),
        compiler_params=pltpu.CompilerParams(
            collective_id=0, has_side_effects=True, vmem_limit_bytes=60 << 20
        ),
        name="layers",
    )(node_input, graph_ids, edge_src, edge_dst, halo_send, edge_feat, w_proj, w_edge, w_qkv, w_out, w_up,
      w_down, norm_gain.transpose(1, 0, 2), norm_shift.transpose(1, 0, 2), cotangent)
    weights = [shape(w.shape, F32) for w in (w_proj, w_edge, w_qkv, w_out, w_up, w_down)]
    results = pl.pallas_call(
        finish_kernel,
        out_shape=[rows, rows, *weights, norm, norm],
        in_specs=[hbm] * (2 + len(GROUPS)) + [vmem] * 2,
        out_specs=[hbm] * 8 + [vmem] * 2,
        scratch_shapes=[pltpu.VMEM(s.shape, s.dtype) for s in (*groups, rows, rows, *weights)]
        + [pltpu.SemaphoreType.DMA((len(GROUPS) + 2,)), pltpu.SemaphoreType.DMA((14,))],
        compiler_params=pltpu.CompilerParams(vmem_limit_bytes=60 << 20),
        name="gradients",
    )(*outs)
    ggain, gshift = results[8].transpose(1, 0, 2), results[9].transpose(1, 0, 2)
    return (*results[:8], ggain, gshift)


BLOCK_CAP = 2048


def extended_2(block, sides, width):
    for axis, dim in sides:
        count = lax.axis_size(axis)
        forward = [(i, i + 1) for i in range(count - 1)]
        forward.append((count - 1, 0))
        backward = [(target, source) for source, target in forward]
        low = lax.ppermute(
            lax.slice_in_dim(block, block.shape[dim] - width, None, axis=dim), axis, forward
        )
        high = lax.ppermute(lax.slice_in_dim(block, 0, width, axis=dim), axis, backward)
        block = jnp.concatenate([low, block, high], axis=dim)
    return block


def block_length(total_rows, upper_limit):
    for length in range(min(total_rows, upper_limit), 0, -1):
        if total_rows % length == 0:
            return length
    return 1


def outer_product(left, right):
    return lax.dot_general(
        left, right, (((0,), (0,)), ((), ())), preferred_element_type=jnp.float32
    )


def times_transposed(left, weight):
    return lax.dot_general(
        left, weight, (((1,), (1,)), ((), ())), preferred_element_type=jnp.float32
    )


def forward_product(left, weight):
    return jnp.dot(left, weight, preferred_element_type=jnp.float32)


def silu_slope_plain(inputs):
    logistic = jax.nn.sigmoid(inputs)
    return logistic * (1.0 + inputs * (1.0 - logistic))


def normalize(inputs, gain_row, shift_row, node_total):
    batch_mean = lax.psum(jnp.sum(inputs, 0), ("nodes", "rep")) / node_total
    centred = inputs - batch_mean
    batch_var = lax.psum(jnp.sum(centred * centred, 0), ("nodes", "rep")) / node_total
    inv_std = lax.rsqrt(batch_var + NORM_EPS)
    standard = (inputs - batch_mean) * inv_std
    return (standard * gain_row + shift_row, standard, inv_std)


def normalize_back(grad_out, standard, inv_std, gain_row, node_total):
    shift_grad, gain_grad = lax.psum(
        (jnp.sum(grad_out, 0), jnp.sum(grad_out * standard, 0)), ("nodes", "rep")
    )
    grad_in = (
        gain_row
        * inv_std
        * (grad_out - shift_grad / node_total - standard * gain_grad / node_total)
    )
    return (grad_in, gain_grad, shift_grad)


def exchange_sources(outgoing):
    halo_rows = outgoing.shape[0] // 2
    grown = extended_2(outgoing, (("nodes", 0),), halo_rows)
    return jnp.concatenate([grown[:halo_rows], grown[3 * halo_rows :]], 0)


def return_sources(incoming_grad):
    halo_rows = incoming_grad.shape[0] // 2
    grown = extended_2(incoming_grad.astype(jnp.bfloat16), (("nodes", 0),), halo_rows).astype(
        incoming_grad.dtype
    )
    return jnp.concatenate([grown[:halo_rows], grown[3 * halo_rows :]], 0)


def attend_forward(query_rows, key_rows, value_rows, local_graphs, group_graphs):
    row_count = query_rows.shape[0]
    score_scale = HEAD_DIM ** (-0.5)
    queries = query_rows.reshape(row_count, HEADS, HEAD_DIM)

    def add_piece(carried, kv_piece, first_row):
        key_piece, value_piece = kv_piece
        piece_rows = key_piece.shape[0]
        block_len = block_length(piece_rows, BLOCK_CAP)

        def add_block(block_state, block_index):
            row_max, row_sum, accumulated = block_state
            block_start = block_index * block_len
            key_block = lax.dynamic_slice_in_dim(key_piece, block_start, block_len, 0).reshape(
                block_len, HEADS, HEAD_DIM
            )
            value_block = lax.dynamic_slice_in_dim(value_piece, block_start, block_len, 0).reshape(
                block_len, HEADS, HEAD_DIM
            )
            key_graphs = lax.dynamic_slice_in_dim(
                group_graphs, first_row + block_start, block_len, 0
            )
            same_graph = (local_graphs[:, None] == key_graphs[None, :])[None]
            scores = (
                jnp.einsum("qhd,khd->hqk", queries, key_block, preferred_element_type=jnp.float32)
                * score_scale
            )
            scores = jnp.where(same_graph, scores, NEG)
            new_max = jnp.maximum(row_max, jnp.max(scores, 2))
            weights = jnp.where(same_graph, jnp.exp(scores - new_max[:, :, None]), 0.0)
            factor = jnp.exp(row_max - new_max)
            row_sum = row_sum * factor + jnp.sum(weights, 2)
            contrib = jnp.einsum(
                "hqk,khd->qhd",
                weights.astype(jnp.bfloat16),
                value_block,
                preferred_element_type=jnp.float32,
            )
            accumulated = accumulated * jnp.transpose(factor)[:, :, None] + contrib
            return ((new_max, row_sum, accumulated), None)

        carried, _ = lax.scan(add_block, carried, jnp.arange(piece_rows // block_len))
        return carried

    start_state = (
        jnp.full((HEADS, row_count), NEG, jnp.float32),
        jnp.zeros((HEADS, row_count), jnp.float32),
        jnp.zeros((row_count, HEADS, HEAD_DIM), jnp.float32),
    )
    row_max, row_sum, accumulated = add_piece(
        start_state,
        (
            lax.all_gather(key_rows, "nodes", axis=0, tiled=True),
            lax.all_gather(value_rows, "nodes", axis=0, tiled=True),
        ),
        jnp.int32(0),
    )
    attn_raw = accumulated / jnp.transpose(row_sum)[:, :, None]
    log_sum = row_max + jnp.log(row_sum)
    return (attn_raw, log_sum)


def attend_backward(
    query_rows, key_rows, value_rows, grad_low, attn_raw, log_sum, local_graphs, group_graphs
):
    row_count = query_rows.shape[0]
    model_width = HEADS * HEAD_DIM
    score_scale = HEAD_DIM ** (-0.5)
    queries = query_rows.reshape(row_count, HEADS, HEAD_DIM)
    grad_heads = grad_low.reshape(row_count, HEADS, HEAD_DIM)
    row_delta = jnp.einsum("qhd,qhd->hq", grad_heads.astype(jnp.float32), attn_raw)

    def score_block(key_block, value_block, key_graphs):
        same_graph = (local_graphs[:, None] == key_graphs[None, :])[None]
        scores = (
            jnp.einsum("qhd,khd->hqk", queries, key_block, preferred_element_type=jnp.float32)
            * score_scale
        )
        attn_weights = jnp.exp(jnp.where(same_graph, scores - log_sum[:, :, None], NEG))
        grad_weights = jnp.einsum(
            "qhd,khd->hqk", grad_heads, value_block, preferred_element_type=jnp.float32
        )
        grad_scores = (attn_weights * (grad_weights - row_delta[:, :, None])).astype(jnp.bfloat16)
        return (attn_weights, grad_scores)

    def key_terms(attn_weights, grad_scores, block_len):
        grad_keys = (
            jnp.einsum("hqk,qhd->khd", grad_scores, queries, preferred_element_type=jnp.float32)
            * score_scale
        )
        grad_values = jnp.einsum(
            "hqk,qhd->khd",
            attn_weights.astype(jnp.bfloat16),
            grad_heads,
            preferred_element_type=jnp.float32,
        )
        return jnp.concatenate(
            [
                grad_keys.reshape(block_len, model_width),
                grad_values.reshape(block_len, model_width),
            ],
            1,
        )

    def query_term(grad_scores, key_block):
        return (
            jnp.einsum("hqk,khd->qhd", grad_scores, key_block, preferred_element_type=jnp.float32)
            * score_scale
        )

    group_rows = group_graphs.shape[0]

    def add_piece(carried, kv_piece, first_row):
        key_piece, value_piece = kv_piece
        piece_rows = key_piece.shape[0]
        block_len = block_length(piece_rows, BLOCK_CAP)

        def add_block(block_state, block_index):
            grad_query, buffer = block_state
            block_start = block_index * block_len
            key_block = lax.dynamic_slice_in_dim(key_piece, block_start, block_len, 0).reshape(
                block_len, HEADS, HEAD_DIM
            )
            value_block = lax.dynamic_slice_in_dim(value_piece, block_start, block_len, 0).reshape(
                block_len, HEADS, HEAD_DIM
            )
            place = first_row + block_start
            key_graphs = lax.dynamic_slice_in_dim(group_graphs, place, block_len, 0)
            attn_weights, grad_scores = score_block(key_block, value_block, key_graphs)
            grad_query = grad_query + query_term(grad_scores, key_block)
            block_terms = key_terms(attn_weights, grad_scores, block_len)
            current = lax.dynamic_slice_in_dim(buffer, place, block_len, 0)
            buffer = lax.dynamic_update_slice_in_dim(buffer, current + block_terms, place, 0)
            return ((grad_query, buffer), None)

        carried, _ = lax.scan(add_block, carried, jnp.arange(piece_rows // block_len))
        return carried

    start_state = (
        jnp.zeros((row_count, HEADS, HEAD_DIM), jnp.float32),
        jnp.zeros((group_rows, 2 * model_width), jnp.float32),
    )
    grad_query, buffer = add_piece(
        start_state,
        (
            lax.all_gather(key_rows, "nodes", axis=0, tiled=True),
            lax.all_gather(value_rows, "nodes", axis=0, tiled=True),
        ),
        jnp.int32(0),
    )
    grad_kv = lax.psum_scatter(buffer, "nodes", scatter_dimension=0, tiled=True)
    return (
        grad_query.reshape(row_count, model_width),
        grad_kv[:, :model_width],
        grad_kv[:, model_width:],
    )


def layer_forward(
    hidden, params, edge_feat, edge_src, edge_dst, halo_send, local_graphs, group_graphs, node_total
):
    w_proj, w_edge, w_qkv, w_out, w_up, w_down, norm_gains, norm_shifts = params
    row_count, model_width = hidden.shape
    hidden_low = hidden.astype(jnp.bfloat16)
    projected = forward_product(hidden_low, w_proj)
    self_term = projected[:, :model_width]
    dest_term = projected[:, 2 * model_width : 3 * model_width]
    source_rows = jnp.concatenate(
        [projected[:, model_width : 2 * model_width], projected[:, 3 * model_width :]], 1
    ).astype(jnp.bfloat16)
    incoming = exchange_sources(source_rows[halo_send])
    extended = jnp.concatenate([source_rows, incoming], 0)
    edge_rows = extended[edge_src].astype(jnp.float32)
    source_b = edge_rows[:, :model_width]
    source_e = edge_rows[:, model_width:]
    edge_proj = forward_product(edge_feat, w_edge)
    gating = jax.nn.sigmoid(dest_term[edge_dst] + source_e + edge_proj)
    numerator = jax.ops.segment_sum(gating * source_b, edge_dst, row_count)
    denominator = jax.ops.segment_sum(gating, edge_dst, row_count)
    message = self_term + numerator / (denominator + GATE_EPS)
    normed_one, standard_one, inv_one = normalize(
        message, norm_gains[0], norm_shifts[0], node_total
    )
    local_out = hidden + jax.nn.silu(normed_one)
    qkv_low = forward_product(hidden_low, w_qkv).astype(jnp.bfloat16)
    query_rows = qkv_low[:, :model_width]
    key_rows = qkv_low[:, model_width : 2 * model_width]
    value_rows = qkv_low[:, 2 * model_width :]
    attn_raw, log_sum = attend_forward(query_rows, key_rows, value_rows, local_graphs, group_graphs)
    attn_low = attn_raw.reshape(row_count, model_width).astype(jnp.bfloat16)
    attn_proj = forward_product(attn_low, w_out)
    normed_two, standard_two, inv_two = normalize(
        hidden + attn_proj, norm_gains[1], norm_shifts[1], node_total
    )
    mixed = local_out + normed_two
    mixed_low = mixed.astype(jnp.bfloat16)
    up_proj = forward_product(mixed_low, w_up)
    activated = jax.nn.silu(up_proj).astype(jnp.bfloat16)
    down_proj = forward_product(activated, w_down)
    normed_three, standard_three, inv_three = normalize(
        mixed + down_proj, norm_gains[2], norm_shifts[2], node_total
    )
    saved = (
        hidden_low,
        source_b,
        gating,
        numerator,
        denominator,
        normed_one,
        standard_one,
        inv_one,
        query_rows,
        key_rows,
        value_rows,
        attn_raw,
        log_sum,
        attn_low,
        standard_two,
        inv_two,
        mixed_low,
        up_proj,
        activated,
        standard_three,
        inv_three,
    )
    return (normed_three, saved)


def layer_backward(
    grad_out,
    params,
    saved,
    edge_feat,
    edge_src,
    edge_dst,
    halo_send,
    local_graphs,
    group_graphs,
    node_total,
):
    w_proj, w_edge, w_qkv, w_out, w_up, w_down, norm_gains, norm_shifts = params
    (
        hidden_low,
        source_b,
        gating,
        numerator,
        denominator,
        normed_one,
        standard_one,
        inv_one,
        query_rows,
        key_rows,
        value_rows,
        attn_raw,
        log_sum,
        attn_low,
        standard_two,
        inv_two,
        mixed_low,
        up_proj,
        activated,
        standard_three,
        inv_three,
    ) = saved
    row_count, model_width = grad_out.shape
    grad_three, gain_three, shift_three = normalize_back(
        grad_out, standard_three, inv_three, norm_gains[2], node_total
    )
    down_grad = grad_three.astype(jnp.bfloat16)
    grad_w_down = outer_product(activated, down_grad)
    up_grad = (times_transposed(down_grad, w_down) * silu_slope_plain(up_proj)).astype(jnp.bfloat16)
    grad_w_up = outer_product(mixed_low, up_grad)
    grad_mixed = grad_three + times_transposed(up_grad, w_up)
    grad_two, gain_two, shift_two = normalize_back(
        grad_mixed, standard_two, inv_two, norm_gains[1], node_total
    )
    out_grad = grad_two.astype(jnp.bfloat16)
    grad_w_out = outer_product(attn_low, out_grad)
    attn_grad = times_transposed(out_grad, w_out).astype(jnp.bfloat16)
    grad_query, grad_key, grad_value = attend_backward(
        query_rows, key_rows, value_rows, attn_grad, attn_raw, log_sum, local_graphs, group_graphs
    )
    qkv_grad = jnp.concatenate([grad_query, grad_key, grad_value], 1).astype(jnp.bfloat16)
    grad_w_qkv = outer_product(hidden_low, qkv_grad)
    grad_message, gain_one, shift_one = normalize_back(
        grad_mixed * silu_slope_plain(normed_one), standard_one, inv_one, norm_gains[0], node_total
    )
    shifted = denominator + GATE_EPS
    grad_numer = grad_message / shifted
    grad_denom = -grad_message * numerator / (shifted * shifted)
    numer_edge = grad_numer[edge_dst]
    grad_gate = numer_edge * source_b + grad_denom[edge_dst]
    grad_pre_edge = grad_gate * gating * (1.0 - gating)
    edge_grad = grad_pre_edge.astype(jnp.bfloat16)
    grad_w_edge = outer_product(edge_feat, edge_grad)
    grad_dest = jax.ops.segment_sum(grad_pre_edge, edge_dst, row_count)
    grad_extended = jax.ops.segment_sum(
        jnp.concatenate([numer_edge * gating, grad_pre_edge], 1),
        edge_src,
        row_count + halo_send.shape[0],
    )
    returned = return_sources(grad_extended[row_count:])
    grad_source = grad_extended[:row_count].at[halo_send].add(returned)
    proj_grad = jnp.concatenate(
        [grad_message, grad_source[:, :model_width], grad_dest, grad_source[:, model_width:]], 1
    ).astype(jnp.bfloat16)
    grad_w_proj = outer_product(hidden_low, proj_grad)
    grad_hidden = (
        grad_mixed
        + grad_two
        + times_transposed(proj_grad, w_proj)
        + times_transposed(qkv_grad, w_qkv)
    )
    weight_grads = (grad_w_proj, grad_w_edge, grad_w_qkv, grad_w_out, grad_w_up, grad_w_down)
    return (
        grad_hidden,
        weight_grads,
        jnp.stack([gain_one, gain_two, gain_three]),
        jnp.stack([shift_one, shift_two, shift_three]),
    )


def per_device(
    node_input,
    edge_feat,
    graph_ids,
    edge_src,
    edge_dst,
    halo_send,
    w_proj,
    w_edge,
    w_qkv,
    w_out,
    w_up,
    w_down,
    norm_gain,
    norm_shift,
    cotangent,
):
    group_graphs = lax.all_gather(graph_ids, "nodes", axis=0, tiled=True)
    node_total = node_input.shape[0] * lax.axis_size("nodes") * lax.axis_size("rep")
    layer_count = w_proj.shape[0]
    layer_params = [
        (
            w_proj[layer_index],
            w_edge[layer_index],
            w_qkv[layer_index],
            w_out[layer_index],
            w_up[layer_index],
            w_down[layer_index],
            norm_gain[layer_index],
            norm_shift[layer_index],
        )
        for layer_index in range(layer_count)
    ]
    hidden = node_input.astype(jnp.float32)
    saved_all = []
    for layer_index in range(layer_count):
        hidden, saved = layer_forward(
            hidden,
            layer_params[layer_index],
            edge_feat,
            edge_src,
            edge_dst,
            halo_send,
            graph_ids,
            group_graphs,
            node_total,
        )
        saved_all.append(saved)
    grad_hidden = cotangent.astype(jnp.float32)
    weight_parts = [None] * layer_count
    gain_parts = [None] * layer_count
    shift_parts = [None] * layer_count
    for layer_index in range(layer_count - 1, -1, -1):
        (
            grad_hidden,
            weight_parts[layer_index],
            gain_parts[layer_index],
            shift_parts[layer_index],
        ) = layer_backward(
            grad_hidden,
            layer_params[layer_index],
            saved_all[layer_index],
            edge_feat,
            edge_src,
            edge_dst,
            halo_send,
            graph_ids,
            group_graphs,
            node_total,
        )
    proj_local = jnp.stack([weight_parts[layer_index][0] for layer_index in range(layer_count)])
    edge_local = jnp.stack([weight_parts[layer_index][1] for layer_index in range(layer_count)])
    qkv_local = jnp.stack([weight_parts[layer_index][2] for layer_index in range(layer_count)])
    out_local = jnp.stack([weight_parts[layer_index][3] for layer_index in range(layer_count)])
    up_local = jnp.stack([weight_parts[layer_index][4] for layer_index in range(layer_count)])
    down_local = jnp.stack([weight_parts[layer_index][5] for layer_index in range(layer_count)])
    grad_proj, grad_edge, grad_qkv, grad_out, grad_up, grad_down = lax.psum(
        (proj_local, edge_local, qkv_local, out_local, up_local, down_local), ("nodes", "rep")
    )
    return (
        hidden,
        grad_hidden,
        grad_proj,
        grad_edge,
        grad_qkv,
        grad_out,
        grad_up,
        grad_down,
        jnp.stack(gain_parts),
        jnp.stack(shift_parts),
    )


def solution(mesh):
    in_specs = (
        P(("rep", "nodes"), None),
        P(("rep", "nodes"), None),
        P(("rep", "nodes")),
        P(("rep", "nodes")),
        P(("rep", "nodes")),
        P(("rep", "nodes")),
        P(),
        P(),
        P(),
        P(),
        P(),
        P(),
        P(),
        P(),
        P(("rep", "nodes"), None),
    )
    out_specs = (
        P(("rep", "nodes"), None),
        P(("rep", "nodes"), None),
        P(),
        P(),
        P(),
        P(),
        P(),
        P(),
        P(),
        P(),
    )
    N, M = mesh.shape["nodes"], mesh.shape["rep"]
    fused = N in (4, 8) and M % 2 == 0 and 512 % (16 * N * M) == 0
    return jax.shard_map(
        functools.partial(fused_device, N, M) if fused else per_device,
        mesh=mesh, in_specs=in_specs, out_specs=out_specs, check_vma=False,
    )
```

```python
import functools
import math

import jax
import jax.numpy as jnp
from jax import lax
from jax.experimental import pallas as pl
from jax.experimental.pallas import tpu as pltpu
from jax.sharding import PartitionSpec as P

HEADS = 8
HEAD_DIM = 32
NEG = -1e30
NORM_EPS = 1e-05
GATE_EPS = 1e-06
F32, BF16, I32 = jnp.float32, jnp.bfloat16, jnp.int32
MESH = pl.DeviceIdType.MESH
SYNCS = 7
GROUPS = (
    ("early", 1, 0, 2560, ("core", "y", "x", "z")),
    ("conv", 1, 0, 2560, ("core", "y", "x", "z")),
    ("qkv", 1, 0, 1536, ("core", "y", "x", "z")),
    ("early", 0, 0, 2560, ("core", "y", "x", "z")),
    ("conv", 0, 0, 2560, ("core", "y", "nodes")),
    ("qkv", 0, 0, 1024, ("rep", "nodes")),
    ("qkv", 0, 1024, 512, ("nodes", "rep")),
)


def dot(left, right):
    return lax.dot_general(
        left, right, (((1,), (0,)), ((), ())), preferred_element_type=F32
    )


def dot_nt(left, right):
    return lax.dot_general(
        left, right, (((1,), (1,)), ((), ())), preferred_element_type=F32
    )


def dot_tn(left, right):
    return lax.dot_general(
        left, right, (((0,), (0,)), ((), ())), preferred_element_type=F32
    )


def split(value):
    high = value.astype(BF16)
    return high, (value - high.astype(F32)).astype(BF16)


def select_rows(onehot, value):
    high, low = split(value)
    return dot(onehot, high) + dot(onehot, low)


def sigmoid(value):
    return 1.0 / (1.0 + jnp.exp(-value))


def silu_slope(value):
    logistic = sigmoid(value)
    return logistic * (1.0 + value * (1.0 - logistic))


def col_sum(value):
    return jnp.sum(value, axis=0, keepdims=True)


def pack(first, second, third, fourth):
    halves = []
    for row in (first, second, third, fourth):
        halves += [row[:, :128], row[:, 128:]]
    return jnp.concatenate(halves, 0)


def unpack(tile):
    return [
        jnp.concatenate([tile[2 * i : 2 * i + 1], tile[2 * i + 1 : 2 * i + 2]], 1)
        for i in range(4)
    ]


def combine_pair(tiles, count):
    mean = jnp.mean(tiles[:, 0:4], 0)
    off = tiles[:, 0:4] - mean
    return jnp.concatenate([mean, jnp.sum(tiles[:, 4:8] + count * off * off, 0)], 0)


def combine_last(tiles, count):
    mean = jnp.mean(tiles[:, 0:2], 0)
    off = tiles[:, 0:2] - mean
    return jnp.concatenate(
        [
            mean,
            jnp.sum(tiles[:, 2:4], 0),
            jnp.sum(tiles[:, 4:6] + count * off * off, 0),
            jnp.sum(tiles[:, 6:8] + off * tiles[:, 2:4], 0),
        ],
        0,
    )


def combine_sum(tiles, count):
    return jnp.sum(tiles, 0)


class Refs:
    pass


def axis_sizes(N, M):
    return dict(core=2, y=M // 2, x=2, z=N // 2, rep=M, nodes=N)


def scratch_list(N, M, L, R, E):
    NZ, NB, G = N // 2, N // 4, N * R
    D, FF, W, HH = 256, 512, 4 * R, HEADS // 2 * R
    dma = lambda *shape: pltpu.SemaphoreType.DMA(shape)
    vm = lambda dtype, *shape: pltpu.VMEM(shape, dtype)
    names = dict(
        gb=vm(BF16, L, N, R, D),
        xs=vm(BF16, L, N, R, D),
        meta=vm(I32, N, 8, 256),
        ef=vm(BF16, E, D),
        cot=vm(BF16, R, D),
        wp=vm(BF16, L, D, 4 * D),
        we=vm(BF16, L, D, D),
        wqkv=vm(BF16, L, D, 3 * D),
        wo=vm(BF16, L, D, D),
        wu=vm(BF16, L, D, FF),
        wd=vm(BF16, L, FF, D),
        st1=vm(F32, SYNCS, N, 8, 128),
        st2=vm(F32, SYNCS, M, 8, 128),
        gain=vm(F32, L, 8, D),
        shift=vm(F32, L, 8, D),
        ggain=vm(F32, L, 8, D),
        gshift=vm(F32, L, 8, D),
        iv=vm(F32, L, 8, D),
        moff=vm(F32, N, 8, D),
        move=vm(F32, 8, D),
        T=vm(BF16, E, R),
        TT=vm(BF16, R, E),
        S=vm(BF16, E, 256),
        ST=vm(BF16, 256, E),
        efT=vm(BF16, D, E),
        HP=vm(BF16, 32, R),
        HN=vm(BF16, 32, R),
        A=vm(BF16, R, 64),
        bias=vm(F32, R, G),
        ce=vm(F32, L, E, D),
        xf=vm(F32, L + 1, R, D),
        xe=vm(BF16, L, 256, D),
        xeT=vm(BF16, D, 256),
        gate=vm(F32, L, E, D),
        bs=vm(BF16, L, E, D),
        num=vm(F32, L, R, D),
        den=vm(F32, L, R, D),
        z0=vm(F32, L, R, D),
        z1=vm(F32, L, R, D),
        z2=vm(F32, L, R, D),
        kk=vm(BF16, L, G, D),
        vv=vm(BF16, L, G, D),
        kT=vm(BF16, D, G),
        vT=vm(BF16, D, G),
        od=vm(F32, NB, R, D),
        md=vm(F32, NB, R, D),
        ld=vm(F32, NB, R, D),
        rb=vm(F32, L, NB, R, D),
        pst=vm(BF16, L, HEADS * R, G),
        oraw=vm(F32, L, R, D),
        ob=vm(BF16, L, R, D),
        mb=vm(BF16, L, R, D),
        u=vm(F32, L, R, FF),
        g=vm(BF16, L, R, FF),
        dy=vm(F32, R, D),
        dmix=vm(F32, R, D),
        dxo=vm(F32, R, D),
        dob=vm(F32, R, D),
        dq=vm(F32, R, D),
        qm=vm(BF16, L, 2, HH, 128),
        qmT=vm(BF16, 2, 128, HH),
        dom=vm(BF16, HH, 128),
        dss=vm(BF16, HH, W),
        dkv=vm(BF16, 2 * D, W),
        gkv=vm(F32, 2 * D, D),
        dce=vm(BF16, E, D),
        dproj=vm(BF16, 4, 256, D),
        dxs=vm(BF16, L, NZ, 2, R, D),
        rs1=vm(BF16, L, NZ, R, D),
        cs=vm(BF16, L, NZ, R, D),
        rs2=vm(BF16, L, NZ, R, D),
        hs=vm(BF16, L, 2, 32, D),
        hr=vm(BF16, L, 2, 32, D),
        gs_early=vm(BF16, L, 2560, 128),
        gs_conv=vm(BF16, L, 2560, 128),
        gs_qkv=vm(BF16, L, 1536, 128),
    )
    sizes = axis_sizes(N, M)
    for g, (_, _, _, rows, stages) in enumerate(GROUPS):
        names[f"go{g}"] = vm(BF16, rows, 128)
        left = rows
        for k, axis in enumerate(stages):
            left //= sizes[axis]
            names[f"ga{g}_{k}"] = vm(BF16, sizes[axis] - 1, left, 128)
            if k < len(stages) - 1:
                names[f"gh{g}_{k}"] = vm(BF16, left, 128)
    names.update(
        load=dma(10),
        store=dma(2),
        meta_s=dma(1),
        meta_r=dma(1),
        st1_s=dma(SYNCS),
        st1_r=dma(SYNCS),
        st2_s=dma(SYNCS),
        st2_r=dma(SYNCS),
        agc_s=dma(L, NZ),
        agc_r=dma(L, NZ),
        agp_s=dma(L, NZ),
        agp_r=dma(L, NZ),
        rsp_s=dma(L, NZ),
        rsp_r=dma(L, NZ),
        rsc_s=dma(L, NZ),
        rsc_r=dma(L, NZ),
        hal_s=dma(L, 2),
        hal_r=dma(L, 2),
        ar_s=dma(len(GROUPS), 8),
        ar_r=dma(len(GROUPS), 8),
        ar_l=dma(len(GROUPS)),
    )
    return names


IN_NAMES = (
    "x_in", "ids", "edge_src", "edge_dst", "halo", "ef_h", "wp_h", "we_h", "wqkv_h", "wo_h", "wu_h", "wd_h",
    "gain_in", "shift_in", "cot_h",
)
OUT_NAMES = ("out_act", "grad_in", *(f"gout{g}" for g in range(len(GROUPS))), "ggain_out", "gshift_out")


def kernel(N, M, L, names, *args):
    r_ = Refs()
    for name, ref in zip(IN_NAMES + OUT_NAMES + tuple(names), args, strict=True):
        setattr(r_, name, ref)
    R, D = r_.x_in.shape
    E = r_.ef.shape[0]
    NZ, NB, G, W = N // 2, N // 4, N * R, 4 * R
    HK = HEADS // 2
    total = float(N * M * R)
    scale = HEAD_DIM ** -0.5
    me = lax.axis_index("nodes")
    rep = lax.axis_index("rep")
    z = me // 2
    par = me % 2
    partner = 2 * z + (1 - par)
    prev = (me + N - 1) % N
    nxt = (me + 1) % N
    zh, zl = z // 2, z % 2
    z_to = lambda t: 2 * ((zh + t // 2) % NB) + (zl + t % 2) % 2
    z_from = lambda t: 2 * ((zh + NB - t // 2) % NB) + (zl + t % 2) % 2

    def remote(src, dst, s_sem, r_sem, **where):
        return pltpu.make_async_remote_copy(
            src_ref=src, dst_ref=dst, send_sem=s_sem, recv_sem=r_sem,
            device_id=where, device_id_type=MESH,
        )

    def send(src, dst, s_sem, r_sem, **where):
        remote(src, dst, s_sem, r_sem, **where).start()

    def arrive(dst, r_sem):
        remote(dst, dst, r_sem, r_sem, nodes=partner).wait_recv()

    def sent(src, s_sem):
        remote(src, src, s_sem, s_sem, nodes=partner).wait_send()

    def when(condition, *acts):
        @pl.when(condition)
        def _():
            for act in acts:
                act()

    loads = [
        pltpu.make_async_copy(getattr(r_, f"{name}_h"), getattr(r_, name), r_.load.at[i])
        for i, name in enumerate(("ef", "we", "wqkv", "wp", "wo", "wu", "wd", "cot"))
    ]
    own_rows = pltpu.make_async_copy(r_.x_in, r_.gb.at[0, me], r_.load.at[8])
    own_rows.start()
    for load in loads:
        load.start()

    barrier = pltpu.get_barrier_semaphore()
    for d in range(1, N):
        pl.semaphore_signal(barrier, inc=1, device_id={"nodes": (me + d) % N}, device_id_type=MESH)
    for d in range(1, M):
        pl.semaphore_signal(barrier, inc=1, device_id={"rep": (rep + d) % M}, device_id_type=MESH)
    pl.semaphore_wait(barrier, N + M - 2)

    def gather_start(l):
        mine = r_.gb.at[l, me]
        send(mine, mine, r_.agp_s.at[l, 0], r_.agp_r.at[l, 0], nodes=partner)
        for t in range(1, NZ):
            send(mine, mine, r_.agc_s.at[l, t], r_.agc_r.at[l, t], nodes=2 * z_to(t) + par)

    def gather_pass(l, t):
        piece = r_.gb.at[l, 2 * z_from(t) + par]
        arrive(piece, r_.agc_r.at[l, t])
        send(piece, piece, r_.agp_s.at[l, t], r_.agp_r.at[l, t], nodes=partner)

    def gather_take(l, t):
        arrive(r_.gb.at[l, 2 * z_from(t) + 1 - par], r_.agp_r.at[l, t])

    def sync_start(k, tile):
        r_.st1[k, me] = tile
        for d in range(1, N):
            send(r_.st1.at[k, me], r_.st1.at[k, me], r_.st1_s.at[k], r_.st1_r.at[k], nodes=(me + d) % N)

    def sync_finish(k, combine):
        arrive(r_.st1.at[k, 0 : N - 1], r_.st1_r.at[k])
        r_.st2[k, rep] = combine(r_.st1[k], float(R))
        for d in range(1, M):
            send(r_.st2.at[k, rep], r_.st2.at[k, rep], r_.st2_s.at[k], r_.st2_r.at[k], rep=(rep + d) % M)
        arrive(r_.st2.at[k, 0 : M - 1], r_.st2_r.at[k])
        return unpack(combine(r_.st2[k], float(R * N)))

    sizes = axis_sizes(N, M)
    core, row = rep % 2, rep // 2
    places = dict(
        core=(core, lambda t: dict(rep=2 * row + t)),
        y=(row, lambda t: dict(rep=2 * t + core)),
        x=(par, lambda t: dict(nodes=2 * z + t)),
        z=(z, lambda t: dict(nodes=2 * t + par)),
        rep=(rep, lambda t: dict(rep=t)),
        nodes=(me, lambda t: dict(nodes=t)),
    )

    def reduce_step(g, step):
        name, layer, first, rows, stages = GROUPS[g]
        K = len(stages)
        gs, out = getattr(r_, f"gs_{name}").at[layer, first : first + rows], getattr(r_, f"go{g}")
        count, offset = [rows], [0]
        for axis in stages:
            count.append(count[-1] // sizes[axis])
            offset.append(offset[-1] + places[axis][0] * count[-1])
        take = lambda start, size: pl.ds(pl.multiple_of(start, 16), size)
        if 1 <= step <= K:
            k = step - 1
            got = getattr(r_, f"ga{g}_{k}")
            arrive(got, r_.ar_r.at[g, k])
            held = gs if k == 0 else getattr(r_, f"gh{g}_{k - 1}")
            index = places[stages[k]][0]
            acc = held[take(index * count[k + 1], count[k + 1])].astype(F32)
            for slot in range(sizes[stages[k]] - 1):
                acc = acc + got[slot].astype(F32)
            if step < K:
                getattr(r_, f"gh{g}_{k}")[...] = acc.astype(BF16)
            else:
                out[take(offset[K], count[K])] = acc.astype(BF16)
        elif step > K:
            k = 2 * K - step
            arrive(out.at[0 : (sizes[stages[k]] - 1) * count[k + 1]], r_.ar_r.at[g, step - 1])
        if step < K:
            held = gs if step == 0 else getattr(r_, f"gh{g}_{step - 1}")
            index, device = places[stages[step]]
            size = sizes[stages[step]]
            for d in range(1, size):
                to = (index + d) % size
                send(held.at[take(to * count[step + 1], count[step + 1])], getattr(r_, f"ga{g}_{step}").at[d - 1],
                     r_.ar_s.at[g, step], r_.ar_r.at[g, step], **device(to))
        elif step < 2 * K:
            k = 2 * K - 1 - step
            index, device = places[stages[k]]
            size = sizes[stages[k]]
            here = out.at[take(offset[k + 1], count[k + 1])]
            for d in range(1, size):
                send(here, here, r_.ar_s.at[g, step], r_.ar_r.at[g, step], **device((index + d) % size))
        else:
            pltpu.make_async_copy(out, getattr(r_, f"gout{g}"), r_.ar_l.at[g]).start()

    def reduce_drain(g):
        _, _, _, rows, stages = GROUPS[g]
        K, left = len(stages), rows
        out = getattr(r_, f"go{g}")
        for k, axis in enumerate(stages):
            left //= sizes[axis]
            for step in (k, 2 * K - 1 - k):
                sent(out.at[0 : (sizes[axis] - 1) * left], r_.ar_s.at[g, step])
        pltpu.make_async_copy(out, getattr(r_, f"gout{g}"), r_.ar_l.at[g]).wait()

    def put(buf, l, at, value):
        rows = value.shape[0]
        for c in range(value.shape[1] // 128):
            buf[l, at : at + rows] = value[:, 128 * c : 128 * (c + 1)].astype(BF16)
            at += rows
        return at

    lane_head = lax.broadcasted_iota(I32, (R, 128), 1) // HEAD_DIM

    def by_head(parts):
        out = parts[0]
        for k in range(1, HK):
            out = jnp.where(lane_head == k, parts[k], out)
        return out

    r_.meta[me] = jnp.full((8, 256), -1, I32)
    r_.meta[me, 0:1, 0:R] = r_.ids[...].reshape(1, R)
    r_.meta[me, 1:2, 0:48] = r_.halo[...].reshape(1, 48)
    for d in range(1, N):
        send(r_.meta.at[me], r_.meta.at[me], r_.meta_s.at[0], r_.meta_r.at[0], nodes=(me + d) % N)
    own_rows.wait()
    gather_start(0)

    src_row = r_.edge_src[...].reshape(1, E)
    src_row = jnp.where(src_row < R + 24, src_row, src_row + 8)
    dst_row = r_.edge_dst[...].reshape(1, E)
    src_col = jnp.broadcast_to(src_row, (128, E)).T[:, 0:1]
    dst_col = jnp.broadcast_to(dst_row, (128, E)).T[:, 0:1]
    as_mask = lambda cond: cond.astype(F32).astype(BF16)
    r_.T[...] = as_mask(dst_col == lax.broadcasted_iota(I32, (E, R), 1))
    r_.TT[...] = as_mask(dst_row == lax.broadcasted_iota(I32, (R, E), 0))
    r_.S[...] = as_mask(src_col == lax.broadcasted_iota(I32, (E, 256), 1))
    r_.ST[...] = as_mask(src_row == lax.broadcasted_iota(I32, (256, E), 0))
    loads[0].wait()
    r_.efT[...] = r_.ef[...].T
    loads[1].wait()
    for l in range(L):
        r_.ce[l] = dot(r_.ef[...], r_.we[l])
        for k in range(3):
            r_.gain[l, k : k + 1] = r_.gain_in[k, l : l + 1]
            r_.shift[l, k : k + 1] = r_.shift_in[k, l : l + 1]
    r_.xf[0] = r_.gb[0, me].astype(F32)
    r_.moff[...] = jnp.zeros((N, 8, D), F32)
    r_.move[0:1] = jnp.ones((1, D), F32)
    r_.move[1:2] = jnp.zeros((1, D), F32)
    for load in loads[2:]:
        load.wait()

    arrive(r_.meta.at[0 : N - 1], r_.meta_r.at[0])
    id_col = jnp.broadcast_to(r_.meta[me][0:1, 0:R], (128, R)).T[:, 0:1]
    id_row = jnp.concatenate([r_.meta[j][0:1, 0:R] for j in range(N)], 1)
    r_.bias[...] = jnp.where(id_col == id_row, 0.0, NEG)

    def halo_onehot(device, start):
        col = jnp.broadcast_to(r_.meta[device][1:2, 0:128], (128, 128)).T[start : start + 24, 0:1]
        hot = (col == lax.broadcasted_iota(I32, (24, R), 1)).astype(F32)
        return jnp.concatenate([hot, jnp.zeros((8, R), F32)], 0).astype(BF16)

    r_.HP[...] = halo_onehot(prev, 24)
    r_.HN[...] = halo_onehot(nxt, 0)
    r_.A[...] = as_mask(r_.meta[me][1:2, 0:64] == lax.broadcasted_iota(I32, (R, 64), 0))

    factor_exp = scale * math.log2(math.e)

    def prepare_queries(l):
        q = dot(r_.xs[l, me], r_.wqkv[l, :, :D]).astype(BF16).astype(F32)
        for hf in range(2):
            for k in range(HK):
                part = jnp.where(lane_head == k, q[:, 128 * hf : 128 * (hf + 1)], 0.0)
                r_.qm[l, hf, k * R : (k + 1) * R] = part.astype(BF16)

    def head_rows(hf, k, count=1):
        return pl.ds(pl.multiple_of((hf * HK + k) * R, 64), count * R)

    def lane_half(hf):
        return pl.ds(pl.multiple_of(hf * 128, 128), 128)

    def attention_block(l, i, middle):
        half = (zh + NB - i) % NB
        rows = pl.ds(pl.multiple_of(half * W, 128), W)
        x = r_.xs[l, pl.ds(4 * half, 4)].reshape(W, D)
        key = dot(x, r_.wqkv[l, :, D : 2 * D]).astype(BF16)
        r_.kk[l, rows] = key
        r_.kT[:, rows] = key.T
        r_.vv[l, rows] = dot(x, r_.wqkv[l, :, 2 * D :]).astype(BF16)

        def heads(hf, carry):
            lanes = lane_half(hf)
            tops, sums, outs = [], [], []
            for c in range(HK // 2):
                scores = dot(r_.qm[l, hf, 2 * c * R : 2 * (c + 1) * R], r_.kT[lanes, rows])
                for k in range(2):
                    s = scores[k * R : (k + 1) * R] + r_.bias[:, rows]
                    top = jnp.max(s, 1, keepdims=True)
                    e = jnp.exp2((s - top) * factor_exp)
                    tops.append(top)
                    sums.append(jnp.sum(e, 1, keepdims=True))
                    r_.pst[l, head_rows(hf, 2 * c + k), rows] = e.astype(BF16)
                o = dot(r_.pst[l, head_rows(hf, 2 * c, 2), rows], r_.vv[l, rows, lanes])
                outs += [o[0:R], o[R : 2 * R]]
            r_.md[i, :, lanes] = by_head([jnp.broadcast_to(v, (R, 128)) for v in tops])
            r_.ld[i, :, lanes] = by_head([jnp.broadcast_to(v, (R, 128)) for v in sums])
            r_.od[i, :, lanes] = by_head(outs)
            middle(i, hf)
            return carry

        lax.fori_loop(0, 2, heads, 0)

    def attention_end(l):
        top = r_.md[0]
        for i in range(1, NB):
            top = jnp.maximum(top, r_.md[i])
        factors = [jnp.exp2((r_.md[i] - top) * factor_exp) for i in range(NB)]
        inv = 1.0 / sum(factors[i] * r_.ld[i] for i in range(NB))
        o = jnp.zeros((R, D), F32)
        for i in range(NB):
            r_.rb[l, i] = factors[i] * inv
            o = o + factors[i] * inv * r_.od[i]
        r_.oraw[l] = o
        ob = o.astype(BF16)
        r_.ob[l] = ob
        t1 = r_.xf[l] + dot(ob, r_.wo[l])
        r_.z1[l] = t1
        mean1 = col_sum(t1) / R
        return mean1, col_sum((t1 - mean1) * (t1 - mean1))

    def convolution(l):
        xs = r_.xs
        xb = xs[l, me]
        r_.xe[l, 0:R] = xb
        r_.xe[l, R : R + 32] = dot(r_.HP[...], xs[l, prev]).astype(BF16)
        r_.xe[l, R + 32 : R + 64] = dot(r_.HN[...], xs[l, nxt]).astype(BF16)
        xe = r_.xe[l]
        tab_b = dot(xe, r_.wp[l, :, D : 2 * D]).astype(BF16)
        tab_e = dot(xe, r_.wp[l, :, 3 * D :]).astype(BF16)
        pa = dot(xb, r_.wp[l, :, 0:D])
        pd = dot(xb, r_.wp[l, :, 2 * D : 3 * D])
        bs = dot(r_.S[...], tab_b)
        r_.bs[l] = bs.astype(BF16)
        gate = sigmoid(select_rows(r_.T[...], pd) + dot(r_.S[...], tab_e) + r_.ce[l])
        r_.gate[l] = gate
        num = select_rows(r_.TT[...], gate * bs)
        den = select_rows(r_.TT[...], gate)
        r_.num[l] = num
        r_.den[l] = den
        msg = pa + num / (den + GATE_EPS)
        r_.z0[l] = msg

    def forward(l, carry):
        def ready(js):
            for j in js:
                moved = (r_.gb[l, j].astype(F32) + r_.moff[j, 0:1]) * r_.move[0:1] + r_.move[1:2]
                r_.xs[l, j] = moved.astype(BF16)

        r_.xs[l, me] = r_.xf[l].astype(BF16)
        gather_pass(l, 1)
        prepare_queries(l)
        gather_take(l, 0)
        gather_take(l, 1)
        ready([partner, 2 * z_from(1) + par, 2 * z_from(1) + 1 - par])

        def middle(i, hf):
            for t in range(2, NZ):
                when((i == 0) & (hf == t - 2), lambda: gather_pass(l, t))

        def block(i, carry):
            attention_block(l, i, middle)

            @pl.when(i == 0)
            def _():
                for t in range(2, NZ):
                    gather_take(l, t)
                ready([2 * z_from(t) + p for t in range(2, NZ) for p in range(2)])
                convolution(l)

            return carry

        lax.fori_loop(0, NB, block, 0)
        mean1, sq1 = attention_end(l)
        msg = r_.z0[l]
        mean0 = col_sum(msg) / R
        sq0 = col_sum((msg - mean0) * (msg - mean0))
        sync_start(2 * l, pack(mean0, mean1, sq0, sq1))
        mean0, mean1, sq0, sq1 = sync_finish(2 * l, combine_pair)
        inv0 = lax.rsqrt(sq0 / total + NORM_EPS)
        inv1 = lax.rsqrt(sq1 / total + NORM_EPS)
        r_.iv[l, 0:1] = inv0
        r_.iv[l, 1:2] = inv1
        z0 = (r_.z0[l] - mean0) * inv0
        z1 = (r_.z1[l] - mean1) * inv1
        r_.z0[l] = z0
        r_.z1[l] = z1
        n0 = z0 * r_.gain[l, 0:1] + r_.shift[l, 0:1]
        mix = r_.xf[l] + n0 * sigmoid(n0) + z1 * r_.gain[l, 1:2] + r_.shift[l, 1:2]
        mb = mix.astype(BF16)
        r_.mb[l] = mb
        u = dot(mb, r_.wu[l])
        r_.u[l] = u
        g = (u * sigmoid(u)).astype(BF16)
        r_.g[l] = g
        y = mix + dot(g, r_.wd[l])
        r_.z2[l] = y
        mean = col_sum(y) / R
        cent = y - mean
        k = 2 * l + 1
        dy = r_.cot[...].astype(F32)
        sync_start(k, pack(mean, col_sum(dy), col_sum(cent * cent), col_sum(dy * cent)))

        @pl.when(l < L - 1)
        def _():
            r_.gb[l + 1, me] = cent.astype(BF16)
            gather_start(l + 1)

        tot_mean, dy_sum, tot_sq, dy_cent = sync_finish(k, combine_last)
        inv2 = lax.rsqrt(tot_sq / total + NORM_EPS)
        r_.iv[l, 2:3] = inv2
        z2 = (r_.z2[l] - tot_mean) * inv2
        r_.z2[l] = z2
        gain, shift = r_.gain[l, 2:3], r_.shift[l, 2:3]
        r_.xf[l + 1] = z2 * gain + shift
        r_.gshift[l, 2:3] = dy_sum
        r_.ggain[l, 2:3] = dy_cent * inv2
        for j in range(N):
            tile = r_.st1[k, j]
            r_.moff[j, 0:1] = jnp.concatenate([tile[0:1], tile[1:2]], 1) - tot_mean
        r_.move[0:1] = inv2 * gain
        r_.move[1:2] = shift
        return carry

    lax.fori_loop(0, L, forward, 0)
    act_copy = pltpu.make_async_copy(r_.xf.at[L], r_.out_act, r_.store.at[0])
    act_copy.start()

    def back_feed_forward(l, k):
        s2, g2 = r_.gshift[l, 2:3], r_.ggain[l, 2:3]
        d3 = r_.gain[l, 2:3] * r_.iv[l, 2:3] * (r_.dy[...] - s2 / total - r_.z2[l] * (g2 / total))
        db = d3.astype(BF16)
        dub = (dot_nt(db, r_.wd[l]) * silu_slope(r_.u[l])).astype(BF16)
        dmix = d3 + dot_nt(dub, r_.wu[l])
        r_.dmix[...] = dmix
        n0 = r_.z0[l] * r_.gain[l, 0:1] + r_.shift[l, 0:1]
        gy0 = dmix * silu_slope(n0)
        sync_start(k, pack(col_sum(dmix), col_sum(dmix * r_.z1[l]), col_sum(gy0), col_sum(gy0 * r_.z0[l])))
        at = put(r_.gs_early, l, 512, dot_tn(r_.mb[l], dub))
        put(r_.gs_early, l, at, dot_tn(r_.g[l], db))
        r_.vT[...] = r_.vv[l].T
        r_.xeT[...] = r_.xe[l].T
        for hf in range(2):
            r_.qmT[hf] = r_.qm[l, hf].T

    def back_norms(l, k):
        s1, g1, s0, g0 = sync_finish(k, combine_sum)
        r_.gshift[l, 1:2] = s1
        r_.ggain[l, 1:2] = g1
        r_.gshift[l, 0:1] = s0
        r_.ggain[l, 0:1] = g0
        dmix = r_.dmix[...]
        d2 = r_.gain[l, 1:2] * r_.iv[l, 1:2] * (dmix - s1 / total - r_.z1[l] * (g1 / total))
        dab = d2.astype(BF16)
        r_.dxo[...] = dmix + d2
        r_.dob[...] = dot_nt(dab, r_.wo[l]).astype(BF16).astype(F32)
        put(r_.gs_early, l, 0, dot_tn(r_.ob[l], dab))
        r_.gkv[...] = jnp.zeros((2 * D, D), F32)
        r_.dq[...] = jnp.zeros((R, D), F32)

    def back_attention_block(l, i, between):
        t1 = (i + 1) % NB
        half = (zh + t1) % NB
        rows = pl.ds(pl.multiple_of(half * W, 128), W)

        def heads(hf, carry):
            lanes = lane_half(hf)
            dos = r_.dob[:, lanes] * r_.rb[l, (NB - t1) % NB, :, lanes]
            prod = dos * r_.oraw[l, :, lanes]
            for k in range(HK):
                r_.dom[k * R : (k + 1) * R] = jnp.where(lane_head == k, dos, 0.0).astype(BF16)
            parts = []
            for c in range(HK // 2):
                both = slice(2 * c * R, 2 * (c + 1) * R)
                dp = dot(r_.dom[both], r_.vT[lanes, rows])
                for k in range(2):
                    h = 2 * c + k
                    delta = jnp.sum(jnp.where(lane_head == h, prod, 0.0), 1, keepdims=True)
                    ds = r_.pst[l, head_rows(hf, h), rows].astype(F32) * (dp[k * R : (k + 1) * R] - delta)
                    r_.dss[h * R : (h + 1) * R] = ds.astype(BF16)
                part = dot(r_.dss[both], r_.kk[l, rows, lanes])
                parts += [part[0:R], part[R : 2 * R]]
            r_.dq[:, lanes] += by_head(parts)
            dk = dot(r_.qmT[hf], r_.dss[...]) * scale
            r_.dkv[pl.ds(pl.multiple_of(hf * 128, 128), 128)] = dk.astype(BF16)
            dv = dot(r_.dom[...].T, r_.pst[l, head_rows(hf, 0, HK), rows])
            r_.dkv[pl.ds(pl.multiple_of(D + hf * 128, 128), 128)] = dv.astype(BF16)
            between(i, hf)
            return carry

        lax.fori_loop(0, 2, heads, 0)
        dx = dot(r_.wqkv[l, :, D:], r_.dkv[...]).T
        r_.dxs[l, pl.ds(2 * half, 2)] = dx.astype(BF16).reshape(2, 2, R, D)
        for low in range(2):
            zb = 2 * half + low
            send(r_.dxs.at[l, zb, 1 - par], r_.rs1.at[l, zb],
                 r_.rsp_s.at[l, 2 * i + low], r_.rsp_r.at[l, 2 * i + low], nodes=partner)
        r_.gkv[...] += dot(r_.dkv[...], r_.xs[l, pl.ds(4 * half, 4)].reshape(W, D))

    def pass_on(l, i, t):
        zb = z_to(t)
        arrive(r_.rs1.at[l, zb], r_.rsp_r.at[l, 2 * i + zb % 2])
        both = r_.dxs[l, zb, par].astype(F32) + r_.rs1[l, zb].astype(F32)
        r_.cs[l, zb] = both.astype(BF16)
        send(r_.cs.at[l, zb], r_.rs2.at[l, z], r_.rsc_s.at[l, t], r_.rsc_r.at[l, t], nodes=2 * zb + par)

    def back_convolution(l):
        s0, g0 = r_.gshift[l, 0:1], r_.ggain[l, 0:1]
        inv_den = 1.0 / (r_.den[l] + GATE_EPS)
        n0 = r_.z0[l] * r_.gain[l, 0:1] + r_.shift[l, 0:1]
        gy0 = r_.dmix[...] * silu_slope(n0)
        dm = r_.gain[l, 0:1] * r_.iv[l, 0:1] * (gy0 - s0 / total - r_.z0[l] * (g0 / total))
        dnum = dm * inv_den
        dden = -dnum * r_.num[l] * inv_den
        dnum_e = select_rows(r_.T[...], dnum)
        dden_e = select_rows(r_.T[...], dden)
        gate = r_.gate[l]
        dgp = (dnum_e * r_.bs[l].astype(F32) + dden_e) * gate * (1.0 - gate)
        r_.dce[...] = dgp.astype(BF16)
        dpb = select_rows(r_.ST[...], dnum_e * gate).astype(BF16)
        dpe = select_rows(r_.ST[...], dgp).astype(BF16)
        dpd = select_rows(r_.TT[...], dgp).astype(BF16)
        dmb = dm.astype(BF16)
        dxe = dot_nt(dpb, r_.wp[l, :, D : 2 * D]) + dot_nt(dpe, r_.wp[l, :, 3 * D :])
        r_.hs[l, 0] = dxe[R : R + 32].astype(BF16)
        r_.hs[l, 1] = dxe[R + 32 : R + 64].astype(BF16)
        send(r_.hs.at[l, 0], r_.hr.at[l, 1], r_.hal_s.at[l, 0], r_.hal_r.at[l, 0], nodes=prev)
        send(r_.hs.at[l, 1], r_.hr.at[l, 0], r_.hal_s.at[l, 1], r_.hal_r.at[l, 1], nodes=nxt)
        r_.dxo[...] += (
            dxe[0:R]
            + dot_nt(dmb, r_.wp[l, :, 0:D])
            + dot_nt(dpd, r_.wp[l, :, 2 * D : 3 * D])
        )
        r_.dproj[0, 0:R] = dmb
        r_.dproj[1] = dpb
        r_.dproj[2, 0:R] = dpd
        r_.dproj[3] = dpe
        at = 0
        for c in range(4):
            width = R if c % 2 == 0 else 256
            at = put(r_.gs_conv, l, at, dot(r_.xeT[:, 0:width], r_.dproj[c, 0:width]))
        put(r_.gs_conv, l, at, dot(r_.efT[...], r_.dce[...]))

    def back_input(l):
        dx = r_.dxo[...]
        arrive(r_.rs1.at[l, z], r_.rsp_r.at[l, 2 * (NB - 1) + zl])
        dx = dx + r_.dxs[l, z, par].astype(F32) + r_.rs1[l, z].astype(F32)
        for t in range(1, NZ):
            c = z_from(t)
            arrive(r_.rs2.at[l, c], r_.rsc_r.at[l, t])
            dx = dx + r_.rs2[l, c].astype(F32)
        arrive(r_.hr.at[l, 0], r_.hal_r.at[l, 1])
        arrive(r_.hr.at[l, 1], r_.hal_r.at[l, 0])
        back = jnp.concatenate(
            [r_.hr[l, 0].astype(F32)[0:24], r_.hr[l, 1].astype(F32)[0:24], jnp.zeros((16, D), F32)], 0
        )
        return dx + dot(r_.A[...], back.astype(BF16))

    def steps(*pairs):
        return [functools.partial(reduce_step, g, k) for g, k in pairs]

    r_.dy[...] = r_.cot[...].astype(F32)

    def backward(b, carry):
        l = L - 1 - b
        first, last = b == 0, b == L - 1
        k = 4 + 2 * b
        back_feed_forward(l, k)
        back_norms(l, k)
        when(first, *steps((0, 0)))
        when(last, *steps((1, 1), (2, 1), (3, 0), (0, 5)))

        def between(i, hf):
            when(first & (i == 0) & (hf == 0), *steps((0, 1)))
            when(first & (i == 1) & (hf == 0), *steps((0, 3)))
            when(last & (i == 0) & (hf == 0), *steps((3, 1), (0, 6)))
            when(last & (i == 0) & (hf == 1), *steps((1, 2), (2, 2)))
            when(last & (i == 1) & (hf == 0), *steps((3, 3), (1, 4), (2, 4), (4, 1)))
            for t in range(2, NZ):
                when((i == 1) & (hf == 0), functools.partial(pass_on, l, 0, t))

        def block(i, carry):
            back_attention_block(l, i, between)

            @pl.when(i == 0)
            def _():
                when(first, *steps((0, 2)))
                when(last, *steps((3, 2), (0, 7), (1, 3), (2, 3)))
                back_convolution(l)
                when(last, *steps((4, 0)))

            return carry

        lax.fori_loop(0, NB, block, 0)
        dqb = (r_.dq[...] * scale).astype(BF16)
        at = put(r_.gs_qkv, l, 0, dot(r_.xeT[:, 0:R], dqb))
        put(r_.gs_qkv, l, at, r_.gkv[...].T)
        r_.dxo[...] += dot_nt(dqb, r_.wqkv[l, :, 0:D])
        when(first, *steps((0, 4)))
        when(last, *steps((5, 0), (6, 0), (4, 2), (3, 4)))
        pass_on(l, NB - 1, 1)
        when(last, *steps((1, 5), (2, 5)))
        dx = back_input(l)
        r_.dy[...] = dx

        @pl.when(first)
        def _():
            below = L - 2
            zero_row = jnp.zeros((1, D), F32)
            sync_start(5, pack(col_sum(dx), col_sum(dx * r_.z2[below]), zero_row, zero_row))
            for step in steps((1, 0), (2, 0)):
                step()
            s2, g2, _, _ = sync_finish(5, combine_sum)
            r_.gshift[below, 2:3] = s2
            r_.ggain[below, 2:3] = g2

        return carry

    lax.fori_loop(0, L, backward, 0)
    in_copy = pltpu.make_async_copy(r_.dy, r_.grad_in, r_.store.at[1])
    in_copy.start()
    for step in steps(
        (6, 1), (5, 1), (4, 3), (3, 5), (1, 6), (2, 6),
        (6, 2), (5, 2), (4, 4), (3, 6), (1, 7), (2, 7), (0, 8),
        (6, 3), (5, 3), (4, 5), (3, 7), (1, 8), (2, 8),
        (6, 4), (5, 4), (4, 6), (3, 8),
    ):
        step()
    for l in range(L):
        for k in range(3):
            r_.ggain_out[k, l : l + 1] = r_.ggain[l, k : k + 1]
            r_.gshift_out[k, l : l + 1] = r_.gshift[l, k : k + 1]
    for g in range(len(GROUPS)):
        reduce_drain(g)
    sent(r_.meta.at[0 : N - 1], r_.meta_s.at[0])
    for k in range(SYNCS):
        sent(r_.st1.at[k, 0 : N - 1], r_.st1_s.at[k])
        sent(r_.st2.at[k, 0 : M - 1], r_.st2_s.at[k])
    for l in range(L):
        for t in range(NZ):
            sent(r_.gb.at[l, 0], r_.agp_s.at[l, t])
            sent(r_.rs1.at[l, 0], r_.rsp_s.at[l, t])
            if t > 0:
                sent(r_.gb.at[l, 0], r_.agc_s.at[l, t])
                sent(r_.rs1.at[l, 0], r_.rsc_s.at[l, t])
        for side in range(2):
            sent(r_.hs.at[l, 0], r_.hal_s.at[l, side])
    act_copy.wait()
    in_copy.wait()


def finish_kernel(act_h, gin_h, *refs):
    n = len(GROUPS)
    held, (ggain_h, gshift_h), refs = refs[:n], refs[n : n + 2], refs[n + 2 :]
    act_o, gin_o, proj_o, edge_o, qkv_o, out_o, up_o, down_o, ggain_o, gshift_o = refs[:10]
    summed, refs = refs[10 : 10 + n], refs[10 + n :]
    act, gin, proj, edge, qkv, out, up, down, in_sem, out_sem = refs
    loads = [
        pltpu.make_async_copy(src, dst, in_sem.at[i])
        for i, (src, dst) in enumerate(zip(held + (act_h, gin_h), summed + (act, gin), strict=True))
    ]
    for load in loads:
        load.start()
    ggain_o[...] = ggain_h[...]
    gshift_o[...] = gshift_h[...]
    stores = []

    def store(src, dst):
        copy = pltpu.make_async_copy(src, dst, out_sem.at[len(stores)])
        copy.start()
        stores.append(copy)

    def widen(dst, l, g, at, first=0, last=None):
        rows = dst.shape[1]
        for c in range(first, dst.shape[2] // 128 if last is None else last):
            dst[l, :, 128 * c : 128 * (c + 1)] = summed[g][at : at + rows].astype(F32)
            at += rows
        return at

    for g, (name, l, first, rows, _) in enumerate(GROUPS):
        loads[g].wait()
        if name == "early":
            at = widen(out, l, g, 0)
            store(out.at[l], out_o.at[l])
            at = widen(up, l, g, at)
            store(up.at[l], up_o.at[l])
            widen(down, l, g, at)
            store(down.at[l], down_o.at[l])
        elif name == "conv":
            at = widen(proj, l, g, 0)
            store(proj.at[l], proj_o.at[l])
            widen(edge, l, g, at)
            store(edge.at[l], edge_o.at[l])
        else:
            widen(qkv, l, g, 0, first // 256, (first + rows) // 256)
            if first + rows == 1536:
                store(qkv.at[l], qkv_o.at[l])
    for i, (src, dst) in enumerate(((act, act_o), (gin, gin_o))):
        loads[n + i].wait()
        store(src, dst)
    for copy in stores:
        copy.wait()


def fused_device(
    N, M, node_input, edge_feat, graph_ids, edge_src, edge_dst, halo_send, w_proj, w_edge, w_qkv,
    w_out, w_up, w_down, norm_gain, norm_shift, cotangent,
):
    R, D = node_input.shape
    E = edge_feat.shape[0]
    L = w_proj.shape[0]
    names = scratch_list(N, M, L, R, E)
    vmem = pl.BlockSpec(memory_space=pltpu.VMEM)
    hbm = pl.BlockSpec(memory_space=pltpu.HBM)
    shape = jax.ShapeDtypeStruct
    rows = shape((R, D), F32)
    norm = shape((3, L, D), F32)
    groups = [shape((rows_g, 128), BF16) for _, _, _, rows_g, _ in GROUPS]
    outs = pl.pallas_call(
        functools.partial(kernel, N, M, L, tuple(names)),
        out_shape=[rows, rows, *groups, norm, norm],
        in_specs=[hbm] + [vmem] * 4 + [hbm] * 7 + [vmem] * 2 + [hbm],
        out_specs=[hbm] * (2 + len(GROUPS)) + [vmem] * 2,
        scratch_shapes=list(names.values()),
        compiler_params=pltpu.CompilerParams(
            collective_id=0, has_side_effects=True, vmem_limit_bytes=60 << 20
        ),
        name="layers",
    )(node_input, graph_ids, edge_src, edge_dst, halo_send, edge_feat, w_proj, w_edge, w_qkv, w_out, w_up,
      w_down, norm_gain.transpose(1, 0, 2), norm_shift.transpose(1, 0, 2), cotangent)
    weights = [shape(w.shape, F32) for w in (w_proj, w_edge, w_qkv, w_out, w_up, w_down)]
    results = pl.pallas_call(
        finish_kernel,
        out_shape=[rows, rows, *weights, norm, norm],
        in_specs=[hbm] * (2 + len(GROUPS)) + [vmem] * 2,
        out_specs=[hbm] * 8 + [vmem] * 2,
        scratch_shapes=[pltpu.VMEM(s.shape, s.dtype) for s in (*groups, rows, rows, *weights)]
        + [pltpu.SemaphoreType.DMA((len(GROUPS) + 2,)), pltpu.SemaphoreType.DMA((14,))],
        compiler_params=pltpu.CompilerParams(vmem_limit_bytes=60 << 20),
        name="gradients",
    )(*outs)
    ggain, gshift = results[8].transpose(1, 0, 2), results[9].transpose(1, 0, 2)
    return (*results[:8], ggain, gshift)


BLOCK_CAP = 2048


def extended_2(block, sides, width):
    for axis, dim in sides:
        count = lax.axis_size(axis)
        forward = [(i, i + 1) for i in range(count - 1)]
        forward.append((count - 1, 0))
        backward = [(target, source) for source, target in forward]
        low = lax.ppermute(
            lax.slice_in_dim(block, block.shape[dim] - width, None, axis=dim), axis, forward
        )
        high = lax.ppermute(lax.slice_in_dim(block, 0, width, axis=dim), axis, backward)
        block = jnp.concatenate([low, block, high], axis=dim)
    return block


def block_length(total_rows, upper_limit):
    for length in range(min(total_rows, upper_limit), 0, -1):
        if total_rows % length == 0:
            return length
    return 1


def outer_product(left, right):
    return lax.dot_general(
        left, right, (((0,), (0,)), ((), ())), preferred_element_type=jnp.float32
    )


def times_transposed(left, weight):
    return lax.dot_general(
        left, weight, (((1,), (1,)), ((), ())), preferred_element_type=jnp.float32
    )


def forward_product(left, weight):
    return jnp.dot(left, weight, preferred_element_type=jnp.float32)


def silu_slope_plain(inputs):
    logistic = jax.nn.sigmoid(inputs)
    return logistic * (1.0 + inputs * (1.0 - logistic))


def normalize(inputs, gain_row, shift_row, node_total):
    batch_mean = lax.psum(jnp.sum(inputs, 0), ("nodes", "rep")) / node_total
    centred = inputs - batch_mean
    batch_var = lax.psum(jnp.sum(centred * centred, 0), ("nodes", "rep")) / node_total
    inv_std = lax.rsqrt(batch_var + NORM_EPS)
    standard = (inputs - batch_mean) * inv_std
    return (standard * gain_row + shift_row, standard, inv_std)


def normalize_back(grad_out, standard, inv_std, gain_row, node_total):
    shift_grad, gain_grad = lax.psum(
        (jnp.sum(grad_out, 0), jnp.sum(grad_out * standard, 0)), ("nodes", "rep")
    )
    grad_in = (
        gain_row
        * inv_std
        * (grad_out - shift_grad / node_total - standard * gain_grad / node_total)
    )
    return (grad_in, gain_grad, shift_grad)


def exchange_sources(outgoing):
    halo_rows = outgoing.shape[0] // 2
    grown = extended_2(outgoing, (("nodes", 0),), halo_rows)
    return jnp.concatenate([grown[:halo_rows], grown[3 * halo_rows :]], 0)


def return_sources(incoming_grad):
    halo_rows = incoming_grad.shape[0] // 2
    grown = extended_2(incoming_grad.astype(jnp.bfloat16), (("nodes", 0),), halo_rows).astype(
        incoming_grad.dtype
    )
    return jnp.concatenate([grown[:halo_rows], grown[3 * halo_rows :]], 0)


def attend_forward(query_rows, key_rows, value_rows, local_graphs, group_graphs):
    row_count = query_rows.shape[0]
    score_scale = HEAD_DIM ** (-0.5)
    queries = query_rows.reshape(row_count, HEADS, HEAD_DIM)

    def add_piece(carried, kv_piece, first_row):
        key_piece, value_piece = kv_piece
        piece_rows = key_piece.shape[0]
        block_len = block_length(piece_rows, BLOCK_CAP)

        def add_block(block_state, block_index):
            row_max, row_sum, accumulated = block_state
            block_start = block_index * block_len
            key_block = lax.dynamic_slice_in_dim(key_piece, block_start, block_len, 0).reshape(
                block_len, HEADS, HEAD_DIM
            )
            value_block = lax.dynamic_slice_in_dim(value_piece, block_start, block_len, 0).reshape(
                block_len, HEADS, HEAD_DIM
            )
            key_graphs = lax.dynamic_slice_in_dim(
                group_graphs, first_row + block_start, block_len, 0
            )
            same_graph = (local_graphs[:, None] == key_graphs[None, :])[None]
            scores = (
                jnp.einsum("qhd,khd->hqk", queries, key_block, preferred_element_type=jnp.float32)
                * score_scale
            )
            scores = jnp.where(same_graph, scores, NEG)
            new_max = jnp.maximum(row_max, jnp.max(scores, 2))
            weights = jnp.where(same_graph, jnp.exp(scores - new_max[:, :, None]), 0.0)
            factor = jnp.exp(row_max - new_max)
            row_sum = row_sum * factor + jnp.sum(weights, 2)
            contrib = jnp.einsum(
                "hqk,khd->qhd",
                weights.astype(jnp.bfloat16),
                value_block,
                preferred_element_type=jnp.float32,
            )
            accumulated = accumulated * jnp.transpose(factor)[:, :, None] + contrib
            return ((new_max, row_sum, accumulated), None)

        carried, _ = lax.scan(add_block, carried, jnp.arange(piece_rows // block_len))
        return carried

    start_state = (
        jnp.full((HEADS, row_count), NEG, jnp.float32),
        jnp.zeros((HEADS, row_count), jnp.float32),
        jnp.zeros((row_count, HEADS, HEAD_DIM), jnp.float32),
    )
    row_max, row_sum, accumulated = add_piece(
        start_state,
        (
            lax.all_gather(key_rows, "nodes", axis=0, tiled=True),
            lax.all_gather(value_rows, "nodes", axis=0, tiled=True),
        ),
        jnp.int32(0),
    )
    attn_raw = accumulated / jnp.transpose(row_sum)[:, :, None]
    log_sum = row_max + jnp.log(row_sum)
    return (attn_raw, log_sum)


def attend_backward(
    query_rows, key_rows, value_rows, grad_low, attn_raw, log_sum, local_graphs, group_graphs
):
    row_count = query_rows.shape[0]
    model_width = HEADS * HEAD_DIM
    score_scale = HEAD_DIM ** (-0.5)
    queries = query_rows.reshape(row_count, HEADS, HEAD_DIM)
    grad_heads = grad_low.reshape(row_count, HEADS, HEAD_DIM)
    row_delta = jnp.einsum("qhd,qhd->hq", grad_heads.astype(jnp.float32), attn_raw)

    def score_block(key_block, value_block, key_graphs):
        same_graph = (local_graphs[:, None] == key_graphs[None, :])[None]
        scores = (
            jnp.einsum("qhd,khd->hqk", queries, key_block, preferred_element_type=jnp.float32)
            * score_scale
        )
        attn_weights = jnp.exp(jnp.where(same_graph, scores - log_sum[:, :, None], NEG))
        grad_weights = jnp.einsum(
            "qhd,khd->hqk", grad_heads, value_block, preferred_element_type=jnp.float32
        )
        grad_scores = (attn_weights * (grad_weights - row_delta[:, :, None])).astype(jnp.bfloat16)
        return (attn_weights, grad_scores)

    def key_terms(attn_weights, grad_scores, block_len):
        grad_keys = (
            jnp.einsum("hqk,qhd->khd", grad_scores, queries, preferred_element_type=jnp.float32)
            * score_scale
        )
        grad_values = jnp.einsum(
            "hqk,qhd->khd",
            attn_weights.astype(jnp.bfloat16),
            grad_heads,
            preferred_element_type=jnp.float32,
        )
        return jnp.concatenate(
            [
                grad_keys.reshape(block_len, model_width),
                grad_values.reshape(block_len, model_width),
            ],
            1,
        )

    def query_term(grad_scores, key_block):
        return (
            jnp.einsum("hqk,khd->qhd", grad_scores, key_block, preferred_element_type=jnp.float32)
            * score_scale
        )

    group_rows = group_graphs.shape[0]

    def add_piece(carried, kv_piece, first_row):
        key_piece, value_piece = kv_piece
        piece_rows = key_piece.shape[0]
        block_len = block_length(piece_rows, BLOCK_CAP)

        def add_block(block_state, block_index):
            grad_query, buffer = block_state
            block_start = block_index * block_len
            key_block = lax.dynamic_slice_in_dim(key_piece, block_start, block_len, 0).reshape(
                block_len, HEADS, HEAD_DIM
            )
            value_block = lax.dynamic_slice_in_dim(value_piece, block_start, block_len, 0).reshape(
                block_len, HEADS, HEAD_DIM
            )
            place = first_row + block_start
            key_graphs = lax.dynamic_slice_in_dim(group_graphs, place, block_len, 0)
            attn_weights, grad_scores = score_block(key_block, value_block, key_graphs)
            grad_query = grad_query + query_term(grad_scores, key_block)
            block_terms = key_terms(attn_weights, grad_scores, block_len)
            current = lax.dynamic_slice_in_dim(buffer, place, block_len, 0)
            buffer = lax.dynamic_update_slice_in_dim(buffer, current + block_terms, place, 0)
            return ((grad_query, buffer), None)

        carried, _ = lax.scan(add_block, carried, jnp.arange(piece_rows // block_len))
        return carried

    start_state = (
        jnp.zeros((row_count, HEADS, HEAD_DIM), jnp.float32),
        jnp.zeros((group_rows, 2 * model_width), jnp.float32),
    )
    grad_query, buffer = add_piece(
        start_state,
        (
            lax.all_gather(key_rows, "nodes", axis=0, tiled=True),
            lax.all_gather(value_rows, "nodes", axis=0, tiled=True),
        ),
        jnp.int32(0),
    )
    grad_kv = lax.psum_scatter(buffer, "nodes", scatter_dimension=0, tiled=True)
    return (
        grad_query.reshape(row_count, model_width),
        grad_kv[:, :model_width],
        grad_kv[:, model_width:],
    )


def layer_forward(
    hidden, params, edge_feat, edge_src, edge_dst, halo_send, local_graphs, group_graphs, node_total
):
    w_proj, w_edge, w_qkv, w_out, w_up, w_down, norm_gains, norm_shifts = params
    row_count, model_width = hidden.shape
    hidden_low = hidden.astype(jnp.bfloat16)
    projected = forward_product(hidden_low, w_proj)
    self_term = projected[:, :model_width]
    dest_term = projected[:, 2 * model_width : 3 * model_width]
    source_rows = jnp.concatenate(
        [projected[:, model_width : 2 * model_width], projected[:, 3 * model_width :]], 1
    ).astype(jnp.bfloat16)
    incoming = exchange_sources(source_rows[halo_send])
    extended = jnp.concatenate([source_rows, incoming], 0)
    edge_rows = extended[edge_src].astype(jnp.float32)
    source_b = edge_rows[:, :model_width]
    source_e = edge_rows[:, model_width:]
    edge_proj = forward_product(edge_feat, w_edge)
    gating = jax.nn.sigmoid(dest_term[edge_dst] + source_e + edge_proj)
    numerator = jax.ops.segment_sum(gating * source_b, edge_dst, row_count)
    denominator = jax.ops.segment_sum(gating, edge_dst, row_count)
    message = self_term + numerator / (denominator + GATE_EPS)
    normed_one, standard_one, inv_one = normalize(
        message, norm_gains[0], norm_shifts[0], node_total
    )
    local_out = hidden + jax.nn.silu(normed_one)
    qkv_low = forward_product(hidden_low, w_qkv).astype(jnp.bfloat16)
    query_rows = qkv_low[:, :model_width]
    key_rows = qkv_low[:, model_width : 2 * model_width]
    value_rows = qkv_low[:, 2 * model_width :]
    attn_raw, log_sum = attend_forward(query_rows, key_rows, value_rows, local_graphs, group_graphs)
    attn_low = attn_raw.reshape(row_count, model_width).astype(jnp.bfloat16)
    attn_proj = forward_product(attn_low, w_out)
    normed_two, standard_two, inv_two = normalize(
        hidden + attn_proj, norm_gains[1], norm_shifts[1], node_total
    )
    mixed = local_out + normed_two
    mixed_low = mixed.astype(jnp.bfloat16)
    up_proj = forward_product(mixed_low, w_up)
    activated = jax.nn.silu(up_proj).astype(jnp.bfloat16)
    down_proj = forward_product(activated, w_down)
    normed_three, standard_three, inv_three = normalize(
        mixed + down_proj, norm_gains[2], norm_shifts[2], node_total
    )
    saved = (
        hidden_low,
        source_b,
        gating,
        numerator,
        denominator,
        normed_one,
        standard_one,
        inv_one,
        query_rows,
        key_rows,
        value_rows,
        attn_raw,
        log_sum,
        attn_low,
        standard_two,
        inv_two,
        mixed_low,
        up_proj,
        activated,
        standard_three,
        inv_three,
    )
    return (normed_three, saved)


def layer_backward(
    grad_out,
    params,
    saved,
    edge_feat,
    edge_src,
    edge_dst,
    halo_send,
    local_graphs,
    group_graphs,
    node_total,
):
    w_proj, w_edge, w_qkv, w_out, w_up, w_down, norm_gains, norm_shifts = params
    (
        hidden_low,
        source_b,
        gating,
        numerator,
        denominator,
        normed_one,
        standard_one,
        inv_one,
        query_rows,
        key_rows,
        value_rows,
        attn_raw,
        log_sum,
        attn_low,
        standard_two,
        inv_two,
        mixed_low,
        up_proj,
        activated,
        standard_three,
        inv_three,
    ) = saved
    row_count, model_width = grad_out.shape
    grad_three, gain_three, shift_three = normalize_back(
        grad_out, standard_three, inv_three, norm_gains[2], node_total
    )
    down_grad = grad_three.astype(jnp.bfloat16)
    grad_w_down = outer_product(activated, down_grad)
    up_grad = (times_transposed(down_grad, w_down) * silu_slope_plain(up_proj)).astype(jnp.bfloat16)
    grad_w_up = outer_product(mixed_low, up_grad)
    grad_mixed = grad_three + times_transposed(up_grad, w_up)
    grad_two, gain_two, shift_two = normalize_back(
        grad_mixed, standard_two, inv_two, norm_gains[1], node_total
    )
    out_grad = grad_two.astype(jnp.bfloat16)
    grad_w_out = outer_product(attn_low, out_grad)
    attn_grad = times_transposed(out_grad, w_out).astype(jnp.bfloat16)
    grad_query, grad_key, grad_value = attend_backward(
        query_rows, key_rows, value_rows, attn_grad, attn_raw, log_sum, local_graphs, group_graphs
    )
    qkv_grad = jnp.concatenate([grad_query, grad_key, grad_value], 1).astype(jnp.bfloat16)
    grad_w_qkv = outer_product(hidden_low, qkv_grad)
    grad_message, gain_one, shift_one = normalize_back(
        grad_mixed * silu_slope_plain(normed_one), standard_one, inv_one, norm_gains[0], node_total
    )
    shifted = denominator + GATE_EPS
    grad_numer = grad_message / shifted
    grad_denom = -grad_message * numerator / (shifted * shifted)
    numer_edge = grad_numer[edge_dst]
    grad_gate = numer_edge * source_b + grad_denom[edge_dst]
    grad_pre_edge = grad_gate * gating * (1.0 - gating)
    edge_grad = grad_pre_edge.astype(jnp.bfloat16)
    grad_w_edge = outer_product(edge_feat, edge_grad)
    grad_dest = jax.ops.segment_sum(grad_pre_edge, edge_dst, row_count)
    grad_extended = jax.ops.segment_sum(
        jnp.concatenate([numer_edge * gating, grad_pre_edge], 1),
        edge_src,
        row_count + halo_send.shape[0],
    )
    returned = return_sources(grad_extended[row_count:])
    grad_source = grad_extended[:row_count].at[halo_send].add(returned)
    proj_grad = jnp.concatenate(
        [grad_message, grad_source[:, :model_width], grad_dest, grad_source[:, model_width:]], 1
    ).astype(jnp.bfloat16)
    grad_w_proj = outer_product(hidden_low, proj_grad)
    grad_hidden = (
        grad_mixed
        + grad_two
        + times_transposed(proj_grad, w_proj)
        + times_transposed(qkv_grad, w_qkv)
    )
    weight_grads = (grad_w_proj, grad_w_edge, grad_w_qkv, grad_w_out, grad_w_up, grad_w_down)
    return (
        grad_hidden,
        weight_grads,
        jnp.stack([gain_one, gain_two, gain_three]),
        jnp.stack([shift_one, shift_two, shift_three]),
    )


def per_device(
    node_input,
    edge_feat,
    graph_ids,
    edge_src,
    edge_dst,
    halo_send,
    w_proj,
    w_edge,
    w_qkv,
    w_out,
    w_up,
    w_down,
    norm_gain,
    norm_shift,
    cotangent,
):
    group_graphs = lax.all_gather(graph_ids, "nodes", axis=0, tiled=True)
    node_total = node_input.shape[0] * lax.axis_size("nodes") * lax.axis_size("rep")
    layer_count = w_proj.shape[0]
    layer_params = [
        (
            w_proj[layer_index],
            w_edge[layer_index],
            w_qkv[layer_index],
            w_out[layer_index],
            w_up[layer_index],
            w_down[layer_index],
            norm_gain[layer_index],
            norm_shift[layer_index],
        )
        for layer_index in range(layer_count)
    ]
    hidden = node_input.astype(jnp.float32)
    saved_all = []
    for layer_index in range(layer_count):
        hidden, saved = layer_forward(
            hidden,
            layer_params[layer_index],
            edge_feat,
            edge_src,
            edge_dst,
            halo_send,
            graph_ids,
            group_graphs,
            node_total,
        )
        saved_all.append(saved)
    grad_hidden = cotangent.astype(jnp.float32)
    weight_parts = [None] * layer_count
    gain_parts = [None] * layer_count
    shift_parts = [None] * layer_count
    for layer_index in range(layer_count - 1, -1, -1):
        (
            grad_hidden,
            weight_parts[layer_index],
            gain_parts[layer_index],
            shift_parts[layer_index],
        ) = layer_backward(
            grad_hidden,
            layer_params[layer_index],
            saved_all[layer_index],
            edge_feat,
            edge_src,
            edge_dst,
            halo_send,
            graph_ids,
            group_graphs,
            node_total,
        )
    proj_local = jnp.stack([weight_parts[layer_index][0] for layer_index in range(layer_count)])
    edge_local = jnp.stack([weight_parts[layer_index][1] for layer_index in range(layer_count)])
    qkv_local = jnp.stack([weight_parts[layer_index][2] for layer_index in range(layer_count)])
    out_local = jnp.stack([weight_parts[layer_index][3] for layer_index in range(layer_count)])
    up_local = jnp.stack([weight_parts[layer_index][4] for layer_index in range(layer_count)])
    down_local = jnp.stack([weight_parts[layer_index][5] for layer_index in range(layer_count)])
    grad_proj, grad_edge, grad_qkv, grad_out, grad_up, grad_down = lax.psum(
        (proj_local, edge_local, qkv_local, out_local, up_local, down_local), ("nodes", "rep")
    )
    return (
        hidden,
        grad_hidden,
        grad_proj,
        grad_edge,
        grad_qkv,
        grad_out,
        grad_up,
        grad_down,
        jnp.stack(gain_parts),
        jnp.stack(shift_parts),
    )


def solution(mesh):
    in_specs = (
        P(("rep", "nodes"), None),
        P(("rep", "nodes"), None),
        P(("rep", "nodes")),
        P(("rep", "nodes")),
        P(("rep", "nodes")),
        P(("rep", "nodes")),
        P(),
        P(),
        P(),
        P(),
        P(),
        P(),
        P(),
        P(),
        P(("rep", "nodes"), None),
    )
    out_specs = (
        P(("rep", "nodes"), None),
        P(("rep", "nodes"), None),
        P(),
        P(),
        P(),
        P(),
        P(),
        P(),
        P(),
        P(),
    )
    N, M = mesh.shape["nodes"], mesh.shape["rep"]
    fused = N in (4, 8) and M % 2 == 0 and 512 % (16 * N * M) == 0
    return jax.shard_map(
        functools.partial(fused_device, N, M) if fused else per_device,
        mesh=mesh, in_specs=in_specs, out_specs=out_specs, check_vma=False,
    )
```

```python
import functools
import math

import jax
import jax.numpy as jnp
from jax import lax
from jax.experimental import pallas as pl
from jax.experimental.pallas import tpu as pltpu
from jax.sharding import PartitionSpec as P

HEADS = 8
HEAD_DIM = 32
NEG = -1e30
NORM_EPS = 1e-05
GATE_EPS = 1e-06
F32, BF16, I32 = jnp.float32, jnp.bfloat16, jnp.int32
MESH = pl.DeviceIdType.MESH
SYNCS = 7
GROUPS = (
    ("early", 1, 0, 2560, ("core", "y", "x", "z")),
    ("conv", 1, 0, 2560, ("core", "x", "y", "z")),
    ("qkv", 1, 0, 1536, ("core", "y", "x", "z")),
    ("early", 0, 0, 2560, ("core", "x", "y", "z")),
    ("conv", 0, 0, 2560, ("core", "y", "x", "z")),
    ("qkv", 0, 0, 1536, ("core", "x", "y", "z")),
)


def dot(left, right):
    return lax.dot_general(
        left, right, (((1,), (0,)), ((), ())), preferred_element_type=F32
    )


def dot_nt(left, right):
    return lax.dot_general(
        left, right, (((1,), (1,)), ((), ())), preferred_element_type=F32
    )


def dot_tn(left, right):
    return lax.dot_general(
        left, right, (((0,), (0,)), ((), ())), preferred_element_type=F32
    )


def split(value):
    high = value.astype(BF16)
    return high, (value - high.astype(F32)).astype(BF16)


def select_rows(onehot, value):
    high, low = split(value)
    return dot(onehot, high) + dot(onehot, low)


def sigmoid(value):
    return 1.0 / (1.0 + jnp.exp(-value))


def silu_slope(value):
    logistic = sigmoid(value)
    return logistic * (1.0 + value * (1.0 - logistic))


def col_sum(value):
    return jnp.sum(value, axis=0, keepdims=True)


def pack(first, second, third, fourth):
    halves = []
    for row in (first, second, third, fourth):
        halves += [row[:, :128], row[:, 128:]]
    return jnp.concatenate(halves, 0)


def unpack(tile):
    return [
        jnp.concatenate([tile[2 * i : 2 * i + 1], tile[2 * i + 1 : 2 * i + 2]], 1)
        for i in range(4)
    ]


def combine_pair(tiles, count):
    mean = jnp.mean(tiles[:, 0:4], 0)
    off = tiles[:, 0:4] - mean
    return jnp.concatenate([mean, jnp.sum(tiles[:, 4:8] + count * off * off, 0)], 0)


def combine_last(tiles, count):
    mean = jnp.mean(tiles[:, 0:2], 0)
    off = tiles[:, 0:2] - mean
    return jnp.concatenate(
        [
            mean,
            jnp.sum(tiles[:, 2:4], 0),
            jnp.sum(tiles[:, 4:6] + count * off * off, 0),
            jnp.sum(tiles[:, 6:8] + off * tiles[:, 2:4], 0),
        ],
        0,
    )


def combine_sum(tiles, count):
    return jnp.sum(tiles, 0)


class Refs:
    pass


def axis_sizes(N, M):
    return dict(core=2, y=M // 2, x=2, z=N // 2, rep=M, nodes=N)


def scratch_list(N, M, L, R, E):
    NZ, NB, G = N // 2, N // 4, N * R
    D, FF, W, HH = 256, 512, 4 * R, HEADS // 2 * R
    dma = lambda *shape: pltpu.SemaphoreType.DMA(shape)
    vm = lambda dtype, *shape: pltpu.VMEM(shape, dtype)
    names = dict(
        gb=vm(BF16, L, N, R, D),
        xs=vm(BF16, L, N, R, D),
        meta=vm(I32, N, 8, 256),
        ef=vm(BF16, E, D),
        cot=vm(BF16, R, D),
        wp=vm(BF16, L, D, 4 * D),
        we=vm(BF16, L, D, D),
        wqkv=vm(BF16, L, D, 3 * D),
        wo=vm(BF16, L, D, D),
        wu=vm(BF16, L, D, FF),
        wd=vm(BF16, L, FF, D),
        st1=vm(F32, SYNCS, N, 8, 128),
        st2=vm(F32, SYNCS, M, 8, 128),
        gain=vm(F32, L, 8, D),
        shift=vm(F32, L, 8, D),
        ggain=vm(F32, L, 8, D),
        gshift=vm(F32, L, 8, D),
        iv=vm(F32, L, 8, D),
        moff=vm(F32, N, 8, D),
        move=vm(F32, 8, D),
        T=vm(BF16, E, R),
        TT=vm(BF16, R, E),
        S=vm(BF16, E, 256),
        ST=vm(BF16, 256, E),
        efT=vm(BF16, D, E),
        HP=vm(BF16, 32, R),
        HN=vm(BF16, 32, R),
        A=vm(BF16, R, 64),
        bias=vm(F32, R, G),
        ce=vm(F32, L, E, D),
        xf=vm(F32, L + 1, R, D),
        xe=vm(BF16, L, 256, D),
        xeT=vm(BF16, D, 256),
        gate=vm(F32, L, E, D),
        bs=vm(BF16, L, E, D),
        num=vm(F32, L, R, D),
        den=vm(F32, L, R, D),
        z0=vm(F32, L, R, D),
        z1=vm(F32, L, R, D),
        z2=vm(F32, L, R, D),
        kk=vm(BF16, L, G, D),
        vv=vm(BF16, L, G, D),
        kT=vm(BF16, D, G),
        vT=vm(BF16, D, G),
        od=vm(F32, NB, R, D),
        md=vm(F32, NB, R, D),
        ld=vm(F32, NB, R, D),
        rb=vm(F32, L, NB, R, D),
        pst=vm(BF16, L, HEADS * R, G),
        oraw=vm(F32, L, R, D),
        ob=vm(BF16, L, R, D),
        mb=vm(BF16, L, R, D),
        u=vm(F32, L, R, FF),
        g=vm(BF16, L, R, FF),
        dy=vm(F32, R, D),
        dmix=vm(F32, R, D),
        dxo=vm(F32, R, D),
        dob=vm(F32, R, D),
        dq=vm(F32, R, D),
        qm=vm(BF16, L, 2, HH, 128),
        qmT=vm(BF16, 2, 128, HH),
        dom=vm(BF16, HH, 128),
        dss=vm(BF16, HH, W),
        dkv=vm(BF16, 2 * D, W),
        gkv=vm(F32, 2 * D, D),
        dce=vm(BF16, E, D),
        dproj=vm(BF16, 4, 256, D),
        dxs=vm(BF16, L, NZ, 2, R, D),
        rs1=vm(BF16, L, NZ, R, D),
        cs=vm(BF16, L, NZ, R, D),
        rs2=vm(BF16, L, NZ, R, D),
        hs=vm(BF16, L, 2, 32, D),
        hr=vm(BF16, L, 2, 32, D),
    )
    names.update(
        load=dma(10),
        store=dma(2),
        meta_s=dma(1),
        meta_r=dma(1),
        st1_s=dma(SYNCS),
        st1_r=dma(SYNCS),
        st2_s=dma(SYNCS),
        st2_r=dma(SYNCS),
        agc_s=dma(L, NZ),
        agc_r=dma(L, NZ),
        agp_s=dma(L, NZ),
        agp_r=dma(L, NZ),
        rsp_s=dma(L, NZ),
        rsp_r=dma(L, NZ),
        rsc_s=dma(L, NZ),
        rsc_r=dma(L, NZ),
        hal_s=dma(L, 2),
        hal_r=dma(L, 2),
    )
    return names


IN_NAMES = (
    "x_in", "ids", "edge_src", "edge_dst", "halo", "ef_h", "wp_h", "we_h", "wqkv_h", "wo_h", "wu_h", "wd_h",
    "gain_in", "shift_in", "cot_h",
)
OUT_NAMES = ("out_act", "grad_in", "gs_early", "gs_conv", "gs_qkv", "ggain_out", "gshift_out")


def kernel(N, M, L, names, *args):
    r_ = Refs()
    for name, ref in zip(IN_NAMES + OUT_NAMES + tuple(names), args, strict=True):
        setattr(r_, name, ref)
    R, D = r_.x_in.shape
    E = r_.ef.shape[0]
    NZ, NB, G, W = N // 2, N // 4, N * R, 4 * R
    HK = HEADS // 2
    total = float(N * M * R)
    scale = HEAD_DIM ** -0.5
    me = lax.axis_index("nodes")
    rep = lax.axis_index("rep")
    z = me // 2
    par = me % 2
    partner = 2 * z + (1 - par)
    prev = (me + N - 1) % N
    nxt = (me + 1) % N
    zh, zl = z // 2, z % 2
    z_to = lambda t: 2 * ((zh + t // 2) % NB) + (zl + t % 2) % 2
    z_from = lambda t: 2 * ((zh + NB - t // 2) % NB) + (zl + t % 2) % 2

    def remote(src, dst, s_sem, r_sem, **where):
        return pltpu.make_async_remote_copy(
            src_ref=src, dst_ref=dst, send_sem=s_sem, recv_sem=r_sem,
            device_id=where, device_id_type=MESH,
        )

    def send(src, dst, s_sem, r_sem, **where):
        remote(src, dst, s_sem, r_sem, **where).start()

    def arrive(dst, r_sem):
        remote(dst, dst, r_sem, r_sem, nodes=partner).wait_recv()

    def sent(src, s_sem):
        remote(src, src, s_sem, s_sem, nodes=partner).wait_send()

    def when(condition, *acts):
        @pl.when(condition)
        def _():
            for act in acts:
                act()

    loads = [
        pltpu.make_async_copy(getattr(r_, f"{name}_h"), getattr(r_, name), r_.load.at[i])
        for i, name in enumerate(("ef", "we", "wqkv", "wp", "wo", "wu", "wd", "cot"))
    ]
    own_rows = pltpu.make_async_copy(r_.x_in, r_.gb.at[0, me], r_.load.at[8])
    own_rows.start()
    for load in loads:
        load.start()

    barrier = pltpu.get_barrier_semaphore()
    for d in range(1, N):
        pl.semaphore_signal(barrier, inc=1, device_id={"nodes": (me + d) % N}, device_id_type=MESH)
    for d in range(1, M):
        pl.semaphore_signal(barrier, inc=1, device_id={"rep": (rep + d) % M}, device_id_type=MESH)
    pl.semaphore_wait(barrier, N + M - 2)

    def gather_start(l):
        mine = r_.gb.at[l, me]
        send(mine, mine, r_.agp_s.at[l, 0], r_.agp_r.at[l, 0], nodes=partner)
        for t in range(1, NZ):
            send(mine, mine, r_.agc_s.at[l, t], r_.agc_r.at[l, t], nodes=2 * z_to(t) + par)

    def gather_pass(l, t):
        piece = r_.gb.at[l, 2 * z_from(t) + par]
        arrive(piece, r_.agc_r.at[l, t])
        send(piece, piece, r_.agp_s.at[l, t], r_.agp_r.at[l, t], nodes=partner)

    def gather_take(l, t):
        arrive(r_.gb.at[l, 2 * z_from(t) + 1 - par], r_.agp_r.at[l, t])

    def sync_start(k, tile):
        r_.st1[k, me] = tile
        for d in range(1, N):
            send(r_.st1.at[k, me], r_.st1.at[k, me], r_.st1_s.at[k], r_.st1_r.at[k], nodes=(me + d) % N)

    def sync_finish(k, combine):
        arrive(r_.st1.at[k, 0 : N - 1], r_.st1_r.at[k])
        r_.st2[k, rep] = combine(r_.st1[k], float(R))
        for d in range(1, M):
            send(r_.st2.at[k, rep], r_.st2.at[k, rep], r_.st2_s.at[k], r_.st2_r.at[k], rep=(rep + d) % M)
        arrive(r_.st2.at[k, 0 : M - 1], r_.st2_r.at[k])
        return unpack(combine(r_.st2[k], float(R * N)))

    def put(buf, l, at, value):
        rows = value.shape[0]
        for c in range(value.shape[1] // 128):
            buf[l, at : at + rows] = value[:, 128 * c : 128 * (c + 1)].astype(BF16)
            at += rows
        return at

    lane_head = lax.broadcasted_iota(I32, (R, 128), 1) // HEAD_DIM

    def by_head(parts):
        out = parts[0]
        for k in range(1, HK):
            out = jnp.where(lane_head == k, parts[k], out)
        return out

    r_.meta[me] = jnp.full((8, 256), -1, I32)
    r_.meta[me, 0:1, 0:R] = r_.ids[...].reshape(1, R)
    r_.meta[me, 1:2, 0:48] = r_.halo[...].reshape(1, 48)
    for d in range(1, N):
        send(r_.meta.at[me], r_.meta.at[me], r_.meta_s.at[0], r_.meta_r.at[0], nodes=(me + d) % N)
    own_rows.wait()
    gather_start(0)

    src_row = r_.edge_src[...].reshape(1, E)
    src_row = jnp.where(src_row < R + 24, src_row, src_row + 8)
    dst_row = r_.edge_dst[...].reshape(1, E)
    src_col = jnp.broadcast_to(src_row, (128, E)).T[:, 0:1]
    dst_col = jnp.broadcast_to(dst_row, (128, E)).T[:, 0:1]
    as_mask = lambda cond: cond.astype(F32).astype(BF16)
    r_.T[...] = as_mask(dst_col == lax.broadcasted_iota(I32, (E, R), 1))
    r_.TT[...] = as_mask(dst_row == lax.broadcasted_iota(I32, (R, E), 0))
    r_.S[...] = as_mask(src_col == lax.broadcasted_iota(I32, (E, 256), 1))
    r_.ST[...] = as_mask(src_row == lax.broadcasted_iota(I32, (256, E), 0))
    loads[0].wait()
    r_.efT[...] = r_.ef[...].T
    loads[1].wait()
    for l in range(L):
        r_.ce[l] = dot(r_.ef[...], r_.we[l])
        for k in range(3):
            r_.gain[l, k : k + 1] = r_.gain_in[k, l : l + 1]
            r_.shift[l, k : k + 1] = r_.shift_in[k, l : l + 1]
    r_.xf[0] = r_.gb[0, me].astype(F32)
    r_.moff[...] = jnp.zeros((N, 8, D), F32)
    r_.move[0:1] = jnp.ones((1, D), F32)
    r_.move[1:2] = jnp.zeros((1, D), F32)
    for load in loads[2:]:
        load.wait()

    arrive(r_.meta.at[0 : N - 1], r_.meta_r.at[0])
    id_col = jnp.broadcast_to(r_.meta[me][0:1, 0:R], (128, R)).T[:, 0:1]
    id_row = jnp.concatenate([r_.meta[j][0:1, 0:R] for j in range(N)], 1)
    r_.bias[...] = jnp.where(id_col == id_row, 0.0, NEG)

    def halo_onehot(device, start):
        col = jnp.broadcast_to(r_.meta[device][1:2, 0:128], (128, 128)).T[start : start + 24, 0:1]
        hot = (col == lax.broadcasted_iota(I32, (24, R), 1)).astype(F32)
        return jnp.concatenate([hot, jnp.zeros((8, R), F32)], 0).astype(BF16)

    r_.HP[...] = halo_onehot(prev, 24)
    r_.HN[...] = halo_onehot(nxt, 0)
    r_.A[...] = as_mask(r_.meta[me][1:2, 0:64] == lax.broadcasted_iota(I32, (R, 64), 0))

    factor_exp = scale * math.log2(math.e)

    def prepare_queries(l):
        q = dot(r_.xs[l, me], r_.wqkv[l, :, :D]).astype(BF16).astype(F32)
        for hf in range(2):
            for k in range(HK):
                part = jnp.where(lane_head == k, q[:, 128 * hf : 128 * (hf + 1)], 0.0)
                r_.qm[l, hf, k * R : (k + 1) * R] = part.astype(BF16)

    def head_rows(hf, k, count=1):
        return pl.ds(pl.multiple_of((hf * HK + k) * R, 64), count * R)

    def lane_half(hf):
        return pl.ds(pl.multiple_of(hf * 128, 128), 128)

    def attention_block(l, i, middle):
        half = (zh + NB - i) % NB
        rows = pl.ds(pl.multiple_of(half * W, 128), W)
        x = r_.xs[l, pl.ds(4 * half, 4)].reshape(W, D)
        key = dot(x, r_.wqkv[l, :, D : 2 * D]).astype(BF16)
        r_.kk[l, rows] = key
        r_.kT[:, rows] = key.T
        r_.vv[l, rows] = dot(x, r_.wqkv[l, :, 2 * D :]).astype(BF16)

        def heads(hf, carry):
            lanes = lane_half(hf)
            tops, sums, outs = [], [], []
            for c in range(HK // 2):
                scores = dot(r_.qm[l, hf, 2 * c * R : 2 * (c + 1) * R], r_.kT[lanes, rows])
                for k in range(2):
                    s = scores[k * R : (k + 1) * R] + r_.bias[:, rows]
                    top = jnp.max(s, 1, keepdims=True)
                    e = jnp.exp2((s - top) * factor_exp)
                    tops.append(top)
                    sums.append(jnp.sum(e, 1, keepdims=True))
                    r_.pst[l, head_rows(hf, 2 * c + k), rows] = e.astype(BF16)
                o = dot(r_.pst[l, head_rows(hf, 2 * c, 2), rows], r_.vv[l, rows, lanes])
                outs += [o[0:R], o[R : 2 * R]]
            r_.md[i, :, lanes] = by_head([jnp.broadcast_to(v, (R, 128)) for v in tops])
            r_.ld[i, :, lanes] = by_head([jnp.broadcast_to(v, (R, 128)) for v in sums])
            r_.od[i, :, lanes] = by_head(outs)
            middle(i, hf)
            return carry

        lax.fori_loop(0, 2, heads, 0)

    def attention_end(l):
        top = r_.md[0]
        for i in range(1, NB):
            top = jnp.maximum(top, r_.md[i])
        factors = [jnp.exp2((r_.md[i] - top) * factor_exp) for i in range(NB)]
        inv = 1.0 / sum(factors[i] * r_.ld[i] for i in range(NB))
        o = jnp.zeros((R, D), F32)
        for i in range(NB):
            r_.rb[l, i] = factors[i] * inv
            o = o + factors[i] * inv * r_.od[i]
        r_.oraw[l] = o
        ob = o.astype(BF16)
        r_.ob[l] = ob
        t1 = r_.xf[l] + dot(ob, r_.wo[l])
        r_.z1[l] = t1
        mean1 = col_sum(t1) / R
        return mean1, col_sum((t1 - mean1) * (t1 - mean1))

    def convolution(l):
        xs = r_.xs
        xb = xs[l, me]
        r_.xe[l, 0:R] = xb
        r_.xe[l, R : R + 32] = dot(r_.HP[...], xs[l, prev]).astype(BF16)
        r_.xe[l, R + 32 : R + 64] = dot(r_.HN[...], xs[l, nxt]).astype(BF16)
        xe = r_.xe[l]
        tab_b = dot(xe, r_.wp[l, :, D : 2 * D]).astype(BF16)
        tab_e = dot(xe, r_.wp[l, :, 3 * D :]).astype(BF16)
        pa = dot(xb, r_.wp[l, :, 0:D])
        pd = dot(xb, r_.wp[l, :, 2 * D : 3 * D])
        bs = dot(r_.S[...], tab_b)
        r_.bs[l] = bs.astype(BF16)
        gate = sigmoid(select_rows(r_.T[...], pd) + dot(r_.S[...], tab_e) + r_.ce[l])
        r_.gate[l] = gate
        num = select_rows(r_.TT[...], gate * bs)
        den = select_rows(r_.TT[...], gate)
        r_.num[l] = num
        r_.den[l] = den
        msg = pa + num / (den + GATE_EPS)
        r_.z0[l] = msg

    def forward(l, carry):
        def ready(js):
            for j in js:
                moved = (r_.gb[l, j].astype(F32) + r_.moff[j, 0:1]) * r_.move[0:1] + r_.move[1:2]
                r_.xs[l, j] = moved.astype(BF16)

        r_.xs[l, me] = r_.xf[l].astype(BF16)
        gather_pass(l, 1)
        prepare_queries(l)
        gather_take(l, 0)
        gather_take(l, 1)
        ready([partner, 2 * z_from(1) + par, 2 * z_from(1) + 1 - par])

        def middle(i, hf):
            for t in range(2, NZ):
                when((i == 0) & (hf == t - 2), lambda: gather_pass(l, t))

        def block(i, carry):
            attention_block(l, i, middle)

            @pl.when(i == 0)
            def _():
                for t in range(2, NZ):
                    gather_take(l, t)
                ready([2 * z_from(t) + p for t in range(2, NZ) for p in range(2)])
                convolution(l)

            return carry

        lax.fori_loop(0, NB, block, 0)
        mean1, sq1 = attention_end(l)
        msg = r_.z0[l]
        mean0 = col_sum(msg) / R
        sq0 = col_sum((msg - mean0) * (msg - mean0))
        sync_start(2 * l, pack(mean0, mean1, sq0, sq1))
        mean0, mean1, sq0, sq1 = sync_finish(2 * l, combine_pair)
        inv0 = lax.rsqrt(sq0 / total + NORM_EPS)
        inv1 = lax.rsqrt(sq1 / total + NORM_EPS)
        r_.iv[l, 0:1] = inv0
        r_.iv[l, 1:2] = inv1
        z0 = (r_.z0[l] - mean0) * inv0
        z1 = (r_.z1[l] - mean1) * inv1
        r_.z0[l] = z0
        r_.z1[l] = z1
        n0 = z0 * r_.gain[l, 0:1] + r_.shift[l, 0:1]
        mix = r_.xf[l] + n0 * sigmoid(n0) + z1 * r_.gain[l, 1:2] + r_.shift[l, 1:2]
        mb = mix.astype(BF16)
        r_.mb[l] = mb
        u = dot(mb, r_.wu[l])
        r_.u[l] = u
        g = (u * sigmoid(u)).astype(BF16)
        r_.g[l] = g
        y = mix + dot(g, r_.wd[l])
        r_.z2[l] = y
        mean = col_sum(y) / R
        cent = y - mean
        k = 2 * l + 1
        dy = r_.cot[...].astype(F32)
        sync_start(k, pack(mean, col_sum(dy), col_sum(cent * cent), col_sum(dy * cent)))

        @pl.when(l < L - 1)
        def _():
            r_.gb[l + 1, me] = cent.astype(BF16)
            gather_start(l + 1)

        tot_mean, dy_sum, tot_sq, dy_cent = sync_finish(k, combine_last)
        inv2 = lax.rsqrt(tot_sq / total + NORM_EPS)
        r_.iv[l, 2:3] = inv2
        z2 = (r_.z2[l] - tot_mean) * inv2
        r_.z2[l] = z2
        gain, shift = r_.gain[l, 2:3], r_.shift[l, 2:3]
        r_.xf[l + 1] = z2 * gain + shift
        r_.gshift[l, 2:3] = dy_sum
        r_.ggain[l, 2:3] = dy_cent * inv2
        for j in range(N):
            tile = r_.st1[k, j]
            r_.moff[j, 0:1] = jnp.concatenate([tile[0:1], tile[1:2]], 1) - tot_mean
        r_.move[0:1] = inv2 * gain
        r_.move[1:2] = shift
        return carry

    lax.fori_loop(0, L, forward, 0)
    act_copy = pltpu.make_async_copy(r_.xf.at[L], r_.out_act, r_.store.at[0])
    act_copy.start()

    def back_feed_forward(l, k):
        s2, g2 = r_.gshift[l, 2:3], r_.ggain[l, 2:3]
        d3 = r_.gain[l, 2:3] * r_.iv[l, 2:3] * (r_.dy[...] - s2 / total - r_.z2[l] * (g2 / total))
        db = d3.astype(BF16)
        dub = (dot_nt(db, r_.wd[l]) * silu_slope(r_.u[l])).astype(BF16)
        dmix = d3 + dot_nt(dub, r_.wu[l])
        r_.dmix[...] = dmix
        n0 = r_.z0[l] * r_.gain[l, 0:1] + r_.shift[l, 0:1]
        gy0 = dmix * silu_slope(n0)
        sync_start(k, pack(col_sum(dmix), col_sum(dmix * r_.z1[l]), col_sum(gy0), col_sum(gy0 * r_.z0[l])))
        at = put(r_.gs_early, l, 512, dot_tn(r_.mb[l], dub))
        put(r_.gs_early, l, at, dot_tn(r_.g[l], db))
        r_.vT[...] = r_.vv[l].T
        r_.xeT[...] = r_.xe[l].T
        for hf in range(2):
            r_.qmT[hf] = r_.qm[l, hf].T

    def back_norms(l, k):
        s1, g1, s0, g0 = sync_finish(k, combine_sum)
        r_.gshift[l, 1:2] = s1
        r_.ggain[l, 1:2] = g1
        r_.gshift[l, 0:1] = s0
        r_.ggain[l, 0:1] = g0
        dmix = r_.dmix[...]
        d2 = r_.gain[l, 1:2] * r_.iv[l, 1:2] * (dmix - s1 / total - r_.z1[l] * (g1 / total))
        dab = d2.astype(BF16)
        r_.dxo[...] = dmix + d2
        r_.dob[...] = dot_nt(dab, r_.wo[l]).astype(BF16).astype(F32)
        put(r_.gs_early, l, 0, dot_tn(r_.ob[l], dab))
        r_.gkv[...] = jnp.zeros((2 * D, D), F32)
        r_.dq[...] = jnp.zeros((R, D), F32)

    def back_attention_block(l, i, between):
        t1 = (i + 1) % NB
        half = (zh + t1) % NB
        rows = pl.ds(pl.multiple_of(half * W, 128), W)

        def heads(hf, carry):
            lanes = lane_half(hf)
            dos = r_.dob[:, lanes] * r_.rb[l, (NB - t1) % NB, :, lanes]
            prod = dos * r_.oraw[l, :, lanes]
            for k in range(HK):
                r_.dom[k * R : (k + 1) * R] = jnp.where(lane_head == k, dos, 0.0).astype(BF16)
            parts = []
            for c in range(HK // 2):
                both = slice(2 * c * R, 2 * (c + 1) * R)
                dp = dot(r_.dom[both], r_.vT[lanes, rows])
                for k in range(2):
                    h = 2 * c + k
                    delta = jnp.sum(jnp.where(lane_head == h, prod, 0.0), 1, keepdims=True)
                    ds = r_.pst[l, head_rows(hf, h), rows].astype(F32) * (dp[k * R : (k + 1) * R] - delta)
                    r_.dss[h * R : (h + 1) * R] = ds.astype(BF16)
                part = dot(r_.dss[both], r_.kk[l, rows, lanes])
                parts += [part[0:R], part[R : 2 * R]]
            r_.dq[:, lanes] += by_head(parts)
            dk = dot(r_.qmT[hf], r_.dss[...]) * scale
            r_.dkv[pl.ds(pl.multiple_of(hf * 128, 128), 128)] = dk.astype(BF16)
            dv = dot(r_.dom[...].T, r_.pst[l, head_rows(hf, 0, HK), rows])
            r_.dkv[pl.ds(pl.multiple_of(D + hf * 128, 128), 128)] = dv.astype(BF16)
            between(i, hf)
            return carry

        lax.fori_loop(0, 2, heads, 0)
        dx = dot(r_.wqkv[l, :, D:], r_.dkv[...]).T
        r_.dxs[l, pl.ds(2 * half, 2)] = dx.astype(BF16).reshape(2, 2, R, D)
        for low in range(2):
            zb = 2 * half + low
            send(r_.dxs.at[l, zb, 1 - par], r_.rs1.at[l, zb],
                 r_.rsp_s.at[l, 2 * i + low], r_.rsp_r.at[l, 2 * i + low], nodes=partner)
        r_.gkv[...] += dot(r_.dkv[...], r_.xs[l, pl.ds(4 * half, 4)].reshape(W, D))

    def pass_on(l, i, t):
        zb = z_to(t)
        arrive(r_.rs1.at[l, zb], r_.rsp_r.at[l, 2 * i + zb % 2])
        both = r_.dxs[l, zb, par].astype(F32) + r_.rs1[l, zb].astype(F32)
        r_.cs[l, zb] = both.astype(BF16)
        send(r_.cs.at[l, zb], r_.rs2.at[l, z], r_.rsc_s.at[l, t], r_.rsc_r.at[l, t], nodes=2 * zb + par)

    def back_convolution(l):
        s0, g0 = r_.gshift[l, 0:1], r_.ggain[l, 0:1]
        inv_den = 1.0 / (r_.den[l] + GATE_EPS)
        n0 = r_.z0[l] * r_.gain[l, 0:1] + r_.shift[l, 0:1]
        gy0 = r_.dmix[...] * silu_slope(n0)
        dm = r_.gain[l, 0:1] * r_.iv[l, 0:1] * (gy0 - s0 / total - r_.z0[l] * (g0 / total))
        dnum = dm * inv_den
        dden = -dnum * r_.num[l] * inv_den
        dnum_e = select_rows(r_.T[...], dnum)
        dden_e = select_rows(r_.T[...], dden)
        gate = r_.gate[l]
        dgp = (dnum_e * r_.bs[l].astype(F32) + dden_e) * gate * (1.0 - gate)
        r_.dce[...] = dgp.astype(BF16)
        dpb = select_rows(r_.ST[...], dnum_e * gate).astype(BF16)
        dpe = select_rows(r_.ST[...], dgp).astype(BF16)
        dpd = select_rows(r_.TT[...], dgp).astype(BF16)
        dmb = dm.astype(BF16)
        dxe = dot_nt(dpb, r_.wp[l, :, D : 2 * D]) + dot_nt(dpe, r_.wp[l, :, 3 * D :])
        r_.hs[l, 0] = dxe[R : R + 32].astype(BF16)
        r_.hs[l, 1] = dxe[R + 32 : R + 64].astype(BF16)
        send(r_.hs.at[l, 0], r_.hr.at[l, 1], r_.hal_s.at[l, 0], r_.hal_r.at[l, 0], nodes=prev)
        send(r_.hs.at[l, 1], r_.hr.at[l, 0], r_.hal_s.at[l, 1], r_.hal_r.at[l, 1], nodes=nxt)
        r_.dxo[...] += (
            dxe[0:R]
            + dot_nt(dmb, r_.wp[l, :, 0:D])
            + dot_nt(dpd, r_.wp[l, :, 2 * D : 3 * D])
        )
        r_.dproj[0, 0:R] = dmb
        r_.dproj[1] = dpb
        r_.dproj[2, 0:R] = dpd
        r_.dproj[3] = dpe
        at = 0
        for c in range(4):
            width = R if c % 2 == 0 else 256
            at = put(r_.gs_conv, l, at, dot(r_.xeT[:, 0:width], r_.dproj[c, 0:width]))
        put(r_.gs_conv, l, at, dot(r_.efT[...], r_.dce[...]))

    def back_input(l):
        dx = r_.dxo[...]
        arrive(r_.rs1.at[l, z], r_.rsp_r.at[l, 2 * (NB - 1) + zl])
        dx = dx + r_.dxs[l, z, par].astype(F32) + r_.rs1[l, z].astype(F32)
        for t in range(1, NZ):
            c = z_from(t)
            arrive(r_.rs2.at[l, c], r_.rsc_r.at[l, t])
            dx = dx + r_.rs2[l, c].astype(F32)
        arrive(r_.hr.at[l, 0], r_.hal_r.at[l, 1])
        arrive(r_.hr.at[l, 1], r_.hal_r.at[l, 0])
        back = jnp.concatenate(
            [r_.hr[l, 0].astype(F32)[0:24], r_.hr[l, 1].astype(F32)[0:24], jnp.zeros((16, D), F32)], 0
        )
        return dx + dot(r_.A[...], back.astype(BF16))

    r_.dy[...] = r_.cot[...].astype(F32)

    def backward(b, carry):
        l = L - 1 - b
        first = b == 0
        k = 4 + 2 * b
        back_feed_forward(l, k)
        back_norms(l, k)

        def between(i, hf):
            for t in range(2, NZ):
                when((i == 1) & (hf == 0), functools.partial(pass_on, l, 0, t))

        def block(i, carry):
            back_attention_block(l, i, between)

            @pl.when(i == 0)
            def _():
                back_convolution(l)

            return carry

        lax.fori_loop(0, NB, block, 0)
        dqb = (r_.dq[...] * scale).astype(BF16)
        at = put(r_.gs_qkv, l, 0, dot(r_.xeT[:, 0:R], dqb))
        put(r_.gs_qkv, l, at, r_.gkv[...].T)
        r_.dxo[...] += dot_nt(dqb, r_.wqkv[l, :, 0:D])
        pass_on(l, NB - 1, 1)
        dx = back_input(l)
        r_.dy[...] = dx

        @pl.when(first)
        def _():
            below = L - 2
            zero_row = jnp.zeros((1, D), F32)
            sync_start(5, pack(col_sum(dx), col_sum(dx * r_.z2[below]), zero_row, zero_row))
            s2, g2, _, _ = sync_finish(5, combine_sum)
            r_.gshift[below, 2:3] = s2
            r_.ggain[below, 2:3] = g2

        return carry

    lax.fori_loop(0, L, backward, 0)
    in_copy = pltpu.make_async_copy(r_.dy, r_.grad_in, r_.store.at[1])
    in_copy.start()
    for l in range(L):
        for k in range(3):
            r_.ggain_out[k, l : l + 1] = r_.ggain[l, k : k + 1]
            r_.gshift_out[k, l : l + 1] = r_.gshift[l, k : k + 1]
    sent(r_.meta.at[0 : N - 1], r_.meta_s.at[0])
    for k in range(SYNCS):
        sent(r_.st1.at[k, 0 : N - 1], r_.st1_s.at[k])
        sent(r_.st2.at[k, 0 : M - 1], r_.st2_s.at[k])
    for l in range(L):
        for t in range(NZ):
            sent(r_.gb.at[l, 0], r_.agp_s.at[l, t])
            sent(r_.rs1.at[l, 0], r_.rsp_s.at[l, t])
            if t > 0:
                sent(r_.gb.at[l, 0], r_.agc_s.at[l, t])
                sent(r_.rs1.at[l, 0], r_.rsc_s.at[l, t])
        for side in range(2):
            sent(r_.hs.at[l, 0], r_.hal_s.at[l, side])
    act_copy.wait()
    in_copy.wait()


def reduce_scratch(N, M):
    dma = lambda *shape: pltpu.SemaphoreType.DMA(shape)
    vm = lambda dtype, *shape: pltpu.VMEM(shape, dtype)
    names = dict(
        gs_early=vm(BF16, 2, 2560, 128),
        gs_conv=vm(BF16, 2, 2560, 128),
        gs_qkv=vm(BF16, 2, 1536, 128),
    )
    sizes = axis_sizes(N, M)
    for g, (_, _, _, rows, stages) in enumerate(GROUPS):
        names[f"go{g}"] = vm(BF16, rows, 128)
        left = rows
        for k, axis in enumerate(stages):
            left //= sizes[axis]
            names[f"ga{g}_{k}"] = vm(BF16, sizes[axis] - 1, left, 128)
            if k < len(stages) - 1:
                names[f"gh{g}_{k}"] = vm(BF16, left, 128)
    names.update(load=dma(3), ar_s=dma(len(GROUPS), 8), ar_r=dma(len(GROUPS), 8), ar_l=dma(len(GROUPS)))
    return names


def reduce_kernel(N, M, names, *args):
    r_ = Refs()
    outs = tuple(f"gout{g}" for g in range(len(GROUPS)))
    for name, ref in zip(("early_h", "conv_h", "qkv_h") + outs + tuple(names), args, strict=True):
        setattr(r_, name, ref)
    me = lax.axis_index("nodes")
    rep = lax.axis_index("rep")
    z = me // 2
    par = me % 2
    partner = 2 * z + (1 - par)
    loads = [
        pltpu.make_async_copy(getattr(r_, f"{name}_h"), getattr(r_, f"gs_{name}"), r_.load.at[i])
        for i, name in enumerate(("early", "conv", "qkv"))
    ]
    for load in loads:
        load.start()

    def remote(src, dst, s_sem, r_sem, **where):
        return pltpu.make_async_remote_copy(
            src_ref=src, dst_ref=dst, send_sem=s_sem, recv_sem=r_sem,
            device_id=where, device_id_type=MESH,
        )

    def send(src, dst, s_sem, r_sem, **where):
        remote(src, dst, s_sem, r_sem, **where).start()

    def arrive(dst, r_sem):
        remote(dst, dst, r_sem, r_sem, nodes=partner).wait_recv()

    def sent(src, s_sem):
        remote(src, src, s_sem, s_sem, nodes=partner).wait_send()

    barrier = pltpu.get_barrier_semaphore()
    for d in range(1, N):
        pl.semaphore_signal(barrier, inc=1, device_id={"nodes": (me + d) % N}, device_id_type=MESH)
    for d in range(1, M):
        pl.semaphore_signal(barrier, inc=1, device_id={"rep": (rep + d) % M}, device_id_type=MESH)
    pl.semaphore_wait(barrier, N + M - 2)
    for load in loads:
        load.wait()

    sizes = axis_sizes(N, M)
    core, row = rep % 2, rep // 2
    places = dict(
        core=(core, lambda t: dict(rep=2 * row + t)),
        y=(row, lambda t: dict(rep=2 * t + core)),
        x=(par, lambda t: dict(nodes=2 * z + t)),
        z=(z, lambda t: dict(nodes=2 * t + par)),
        rep=(rep, lambda t: dict(rep=t)),
        nodes=(me, lambda t: dict(nodes=t)),
    )

    def reduce_step(g, step):
        name, layer, first, rows, stages = GROUPS[g]
        K = len(stages)
        gs, out = getattr(r_, f"gs_{name}").at[layer, first : first + rows], getattr(r_, f"go{g}")
        count, offset = [rows], [0]
        for axis in stages:
            count.append(count[-1] // sizes[axis])
            offset.append(offset[-1] + places[axis][0] * count[-1])
        take = lambda start, size: pl.ds(pl.multiple_of(start, 16), size)
        if 1 <= step <= K:
            k = step - 1
            got = getattr(r_, f"ga{g}_{k}")
            arrive(got, r_.ar_r.at[g, k])
            held = gs if k == 0 else getattr(r_, f"gh{g}_{k - 1}")
            index = places[stages[k]][0]
            acc = held[take(index * count[k + 1], count[k + 1])].astype(F32)
            for slot in range(sizes[stages[k]] - 1):
                acc = acc + got[slot].astype(F32)
            if step < K:
                getattr(r_, f"gh{g}_{k}")[...] = acc.astype(BF16)
            else:
                out[take(offset[K], count[K])] = acc.astype(BF16)
        elif step > K:
            k = 2 * K - step
            arrive(out.at[0 : (sizes[stages[k]] - 1) * count[k + 1]], r_.ar_r.at[g, step - 1])
        if step < K:
            held = gs if step == 0 else getattr(r_, f"gh{g}_{step - 1}")
            index, device = places[stages[step]]
            size = sizes[stages[step]]
            for d in range(1, size):
                to = (index + d) % size
                send(held.at[take(to * count[step + 1], count[step + 1])], getattr(r_, f"ga{g}_{step}").at[d - 1],
                     r_.ar_s.at[g, step], r_.ar_r.at[g, step], **device(to))
        elif step < 2 * K:
            k = 2 * K - 1 - step
            index, device = places[stages[k]]
            size = sizes[stages[k]]
            here = out.at[take(offset[k + 1], count[k + 1])]
            for d in range(1, size):
                send(here, here, r_.ar_s.at[g, step], r_.ar_r.at[g, step], **device((index + d) % size))
        else:
            pltpu.make_async_copy(out, getattr(r_, f"gout{g}"), r_.ar_l.at[g]).start()

    def reduce_drain(g):
        _, _, _, rows, stages = GROUPS[g]
        K, left = len(stages), rows
        out = getattr(r_, f"go{g}")
        for k, axis in enumerate(stages):
            left //= sizes[axis]
            for step in (k, 2 * K - 1 - k):
                sent(out.at[0 : (sizes[axis] - 1) * left], r_.ar_s.at[g, step])
        pltpu.make_async_copy(out, getattr(r_, f"gout{g}"), r_.ar_l.at[g]).wait()

    for step in range(2 * 4 + 1):
        for g in range(len(GROUPS)):
            reduce_step(g, step)
    for g in range(len(GROUPS)):
        reduce_drain(g)


def finish_kernel(act_h, gin_h, *refs):
    n = len(GROUPS)
    held, (ggain_h, gshift_h), refs = refs[:n], refs[n : n + 2], refs[n + 2 :]
    act_o, gin_o, proj_o, edge_o, qkv_o, out_o, up_o, down_o, ggain_o, gshift_o = refs[:10]
    summed, refs = refs[10 : 10 + n], refs[10 + n :]
    act, gin, proj, edge, qkv, out, up, down, in_sem, out_sem = refs
    loads = [
        pltpu.make_async_copy(src, dst, in_sem.at[i])
        for i, (src, dst) in enumerate(zip(held + (act_h, gin_h), summed + (act, gin), strict=True))
    ]
    for load in loads:
        load.start()
    ggain_o[...] = ggain_h[...]
    gshift_o[...] = gshift_h[...]
    stores = []

    def store(src, dst):
        copy = pltpu.make_async_copy(src, dst, out_sem.at[len(stores)])
        copy.start()
        stores.append(copy)

    def widen(dst, l, g, at, first=0, last=None):
        rows = dst.shape[1]
        for c in range(first, dst.shape[2] // 128 if last is None else last):
            dst[l, :, 128 * c : 128 * (c + 1)] = summed[g][at : at + rows].astype(F32)
            at += rows
        return at

    for g, (name, l, first, rows, _) in enumerate(GROUPS):
        loads[g].wait()
        if name == "early":
            at = widen(out, l, g, 0)
            store(out.at[l], out_o.at[l])
            at = widen(up, l, g, at)
            store(up.at[l], up_o.at[l])
            widen(down, l, g, at)
            store(down.at[l], down_o.at[l])
        elif name == "conv":
            at = widen(proj, l, g, 0)
            store(proj.at[l], proj_o.at[l])
            widen(edge, l, g, at)
            store(edge.at[l], edge_o.at[l])
        else:
            widen(qkv, l, g, 0, first // 256, (first + rows) // 256)
            if first + rows == 1536:
                store(qkv.at[l], qkv_o.at[l])
    for i, (src, dst) in enumerate(((act, act_o), (gin, gin_o))):
        loads[n + i].wait()
        store(src, dst)
    for copy in stores:
        copy.wait()


def fused_device(
    N, M, node_input, edge_feat, graph_ids, edge_src, edge_dst, halo_send, w_proj, w_edge, w_qkv,
    w_out, w_up, w_down, norm_gain, norm_shift, cotangent,
):
    R, D = node_input.shape
    E = edge_feat.shape[0]
    L = w_proj.shape[0]
    names = scratch_list(N, M, L, R, E)
    vmem = pl.BlockSpec(memory_space=pltpu.VMEM)
    hbm = pl.BlockSpec(memory_space=pltpu.HBM)
    shape = jax.ShapeDtypeStruct
    rows = shape((R, D), F32)
    norm = shape((3, L, D), F32)
    groups = [shape((rows_g, 128), BF16) for _, _, _, rows_g, _ in GROUPS]
    partial = [shape((L, count, 128), BF16) for count in (2560, 2560, 1536)]
    act, gin, early, conv, qkv, ggain, gshift = pl.pallas_call(
        functools.partial(kernel, N, M, L, tuple(names)),
        out_shape=[rows, rows, *partial, norm, norm],
        in_specs=[hbm] + [vmem] * 4 + [hbm] * 7 + [vmem] * 2 + [hbm],
        out_specs=[hbm] * 2 + [vmem] * 5,
        scratch_shapes=list(names.values()),
        compiler_params=pltpu.CompilerParams(
            collective_id=0, has_side_effects=True, vmem_limit_bytes=60 << 20
        ),
        name="layers",
    )(node_input, graph_ids, edge_src, edge_dst, halo_send, edge_feat, w_proj, w_edge, w_qkv, w_out, w_up,
      w_down, norm_gain.transpose(1, 0, 2), norm_shift.transpose(1, 0, 2), cotangent)
    names = reduce_scratch(N, M)
    summed = pl.pallas_call(
        functools.partial(reduce_kernel, N, M, tuple(names)),
        out_shape=groups,
        in_specs=[hbm] * 3,
        out_specs=[hbm] * len(GROUPS),
        scratch_shapes=list(names.values()),
        compiler_params=pltpu.CompilerParams(
            collective_id=1, has_side_effects=True, vmem_limit_bytes=60 << 20
        ),
        name="sums",
    )(early, conv, qkv)
    outs = (act, gin, *summed, ggain, gshift)
    weights = [shape(w.shape, F32) for w in (w_proj, w_edge, w_qkv, w_out, w_up, w_down)]
    results = pl.pallas_call(
        finish_kernel,
        out_shape=[rows, rows, *weights, norm, norm],
        in_specs=[hbm] * (2 + len(GROUPS)) + [vmem] * 2,
        out_specs=[hbm] * 8 + [vmem] * 2,
        scratch_shapes=[pltpu.VMEM(s.shape, s.dtype) for s in (*groups, rows, rows, *weights)]
        + [pltpu.SemaphoreType.DMA((len(GROUPS) + 2,)), pltpu.SemaphoreType.DMA((14,))],
        compiler_params=pltpu.CompilerParams(vmem_limit_bytes=60 << 20),
        name="gradients",
    )(*outs)
    ggain, gshift = results[8].transpose(1, 0, 2), results[9].transpose(1, 0, 2)
    return (*results[:8], ggain, gshift)


BLOCK_CAP = 2048


def extended_2(block, sides, width):
    for axis, dim in sides:
        count = lax.axis_size(axis)
        forward = [(i, i + 1) for i in range(count - 1)]
        forward.append((count - 1, 0))
        backward = [(target, source) for source, target in forward]
        low = lax.ppermute(
            lax.slice_in_dim(block, block.shape[dim] - width, None, axis=dim), axis, forward
        )
        high = lax.ppermute(lax.slice_in_dim(block, 0, width, axis=dim), axis, backward)
        block = jnp.concatenate([low, block, high], axis=dim)
    return block


def block_length(total_rows, upper_limit):
    for length in range(min(total_rows, upper_limit), 0, -1):
        if total_rows % length == 0:
            return length
    return 1


def outer_product(left, right):
    return lax.dot_general(
        left, right, (((0,), (0,)), ((), ())), preferred_element_type=jnp.float32
    )


def times_transposed(left, weight):
    return lax.dot_general(
        left, weight, (((1,), (1,)), ((), ())), preferred_element_type=jnp.float32
    )


def forward_product(left, weight):
    return jnp.dot(left, weight, preferred_element_type=jnp.float32)


def silu_slope_plain(inputs):
    logistic = jax.nn.sigmoid(inputs)
    return logistic * (1.0 + inputs * (1.0 - logistic))


def normalize(inputs, gain_row, shift_row, node_total):
    batch_mean = lax.psum(jnp.sum(inputs, 0), ("nodes", "rep")) / node_total
    centred = inputs - batch_mean
    batch_var = lax.psum(jnp.sum(centred * centred, 0), ("nodes", "rep")) / node_total
    inv_std = lax.rsqrt(batch_var + NORM_EPS)
    standard = (inputs - batch_mean) * inv_std
    return (standard * gain_row + shift_row, standard, inv_std)


def normalize_back(grad_out, standard, inv_std, gain_row, node_total):
    shift_grad, gain_grad = lax.psum(
        (jnp.sum(grad_out, 0), jnp.sum(grad_out * standard, 0)), ("nodes", "rep")
    )
    grad_in = (
        gain_row
        * inv_std
        * (grad_out - shift_grad / node_total - standard * gain_grad / node_total)
    )
    return (grad_in, gain_grad, shift_grad)


def exchange_sources(outgoing):
    halo_rows = outgoing.shape[0] // 2
    grown = extended_2(outgoing, (("nodes", 0),), halo_rows)
    return jnp.concatenate([grown[:halo_rows], grown[3 * halo_rows :]], 0)


def return_sources(incoming_grad):
    halo_rows = incoming_grad.shape[0] // 2
    grown = extended_2(incoming_grad.astype(jnp.bfloat16), (("nodes", 0),), halo_rows).astype(
        incoming_grad.dtype
    )
    return jnp.concatenate([grown[:halo_rows], grown[3 * halo_rows :]], 0)


def attend_forward(query_rows, key_rows, value_rows, local_graphs, group_graphs):
    row_count = query_rows.shape[0]
    score_scale = HEAD_DIM ** (-0.5)
    queries = query_rows.reshape(row_count, HEADS, HEAD_DIM)

    def add_piece(carried, kv_piece, first_row):
        key_piece, value_piece = kv_piece
        piece_rows = key_piece.shape[0]
        block_len = block_length(piece_rows, BLOCK_CAP)

        def add_block(block_state, block_index):
            row_max, row_sum, accumulated = block_state
            block_start = block_index * block_len
            key_block = lax.dynamic_slice_in_dim(key_piece, block_start, block_len, 0).reshape(
                block_len, HEADS, HEAD_DIM
            )
            value_block = lax.dynamic_slice_in_dim(value_piece, block_start, block_len, 0).reshape(
                block_len, HEADS, HEAD_DIM
            )
            key_graphs = lax.dynamic_slice_in_dim(
                group_graphs, first_row + block_start, block_len, 0
            )
            same_graph = (local_graphs[:, None] == key_graphs[None, :])[None]
            scores = (
                jnp.einsum("qhd,khd->hqk", queries, key_block, preferred_element_type=jnp.float32)
                * score_scale
            )
            scores = jnp.where(same_graph, scores, NEG)
            new_max = jnp.maximum(row_max, jnp.max(scores, 2))
            weights = jnp.where(same_graph, jnp.exp(scores - new_max[:, :, None]), 0.0)
            factor = jnp.exp(row_max - new_max)
            row_sum = row_sum * factor + jnp.sum(weights, 2)
            contrib = jnp.einsum(
                "hqk,khd->qhd",
                weights.astype(jnp.bfloat16),
                value_block,
                preferred_element_type=jnp.float32,
            )
            accumulated = accumulated * jnp.transpose(factor)[:, :, None] + contrib
            return ((new_max, row_sum, accumulated), None)

        carried, _ = lax.scan(add_block, carried, jnp.arange(piece_rows // block_len))
        return carried

    start_state = (
        jnp.full((HEADS, row_count), NEG, jnp.float32),
        jnp.zeros((HEADS, row_count), jnp.float32),
        jnp.zeros((row_count, HEADS, HEAD_DIM), jnp.float32),
    )
    row_max, row_sum, accumulated = add_piece(
        start_state,
        (
            lax.all_gather(key_rows, "nodes", axis=0, tiled=True),
            lax.all_gather(value_rows, "nodes", axis=0, tiled=True),
        ),
        jnp.int32(0),
    )
    attn_raw = accumulated / jnp.transpose(row_sum)[:, :, None]
    log_sum = row_max + jnp.log(row_sum)
    return (attn_raw, log_sum)


def attend_backward(
    query_rows, key_rows, value_rows, grad_low, attn_raw, log_sum, local_graphs, group_graphs
):
    row_count = query_rows.shape[0]
    model_width = HEADS * HEAD_DIM
    score_scale = HEAD_DIM ** (-0.5)
    queries = query_rows.reshape(row_count, HEADS, HEAD_DIM)
    grad_heads = grad_low.reshape(row_count, HEADS, HEAD_DIM)
    row_delta = jnp.einsum("qhd,qhd->hq", grad_heads.astype(jnp.float32), attn_raw)

    def score_block(key_block, value_block, key_graphs):
        same_graph = (local_graphs[:, None] == key_graphs[None, :])[None]
        scores = (
            jnp.einsum("qhd,khd->hqk", queries, key_block, preferred_element_type=jnp.float32)
            * score_scale
        )
        attn_weights = jnp.exp(jnp.where(same_graph, scores - log_sum[:, :, None], NEG))
        grad_weights = jnp.einsum(
            "qhd,khd->hqk", grad_heads, value_block, preferred_element_type=jnp.float32
        )
        grad_scores = (attn_weights * (grad_weights - row_delta[:, :, None])).astype(jnp.bfloat16)
        return (attn_weights, grad_scores)

    def key_terms(attn_weights, grad_scores, block_len):
        grad_keys = (
            jnp.einsum("hqk,qhd->khd", grad_scores, queries, preferred_element_type=jnp.float32)
            * score_scale
        )
        grad_values = jnp.einsum(
            "hqk,qhd->khd",
            attn_weights.astype(jnp.bfloat16),
            grad_heads,
            preferred_element_type=jnp.float32,
        )
        return jnp.concatenate(
            [
                grad_keys.reshape(block_len, model_width),
                grad_values.reshape(block_len, model_width),
            ],
            1,
        )

    def query_term(grad_scores, key_block):
        return (
            jnp.einsum("hqk,khd->qhd", grad_scores, key_block, preferred_element_type=jnp.float32)
            * score_scale
        )

    group_rows = group_graphs.shape[0]

    def add_piece(carried, kv_piece, first_row):
        key_piece, value_piece = kv_piece
        piece_rows = key_piece.shape[0]
        block_len = block_length(piece_rows, BLOCK_CAP)

        def add_block(block_state, block_index):
            grad_query, buffer = block_state
            block_start = block_index * block_len
            key_block = lax.dynamic_slice_in_dim(key_piece, block_start, block_len, 0).reshape(
                block_len, HEADS, HEAD_DIM
            )
            value_block = lax.dynamic_slice_in_dim(value_piece, block_start, block_len, 0).reshape(
                block_len, HEADS, HEAD_DIM
            )
            place = first_row + block_start
            key_graphs = lax.dynamic_slice_in_dim(group_graphs, place, block_len, 0)
            attn_weights, grad_scores = score_block(key_block, value_block, key_graphs)
            grad_query = grad_query + query_term(grad_scores, key_block)
            block_terms = key_terms(attn_weights, grad_scores, block_len)
            current = lax.dynamic_slice_in_dim(buffer, place, block_len, 0)
            buffer = lax.dynamic_update_slice_in_dim(buffer, current + block_terms, place, 0)
            return ((grad_query, buffer), None)

        carried, _ = lax.scan(add_block, carried, jnp.arange(piece_rows // block_len))
        return carried

    start_state = (
        jnp.zeros((row_count, HEADS, HEAD_DIM), jnp.float32),
        jnp.zeros((group_rows, 2 * model_width), jnp.float32),
    )
    grad_query, buffer = add_piece(
        start_state,
        (
            lax.all_gather(key_rows, "nodes", axis=0, tiled=True),
            lax.all_gather(value_rows, "nodes", axis=0, tiled=True),
        ),
        jnp.int32(0),
    )
    grad_kv = lax.psum_scatter(buffer, "nodes", scatter_dimension=0, tiled=True)
    return (
        grad_query.reshape(row_count, model_width),
        grad_kv[:, :model_width],
        grad_kv[:, model_width:],
    )


def layer_forward(
    hidden, params, edge_feat, edge_src, edge_dst, halo_send, local_graphs, group_graphs, node_total
):
    w_proj, w_edge, w_qkv, w_out, w_up, w_down, norm_gains, norm_shifts = params
    row_count, model_width = hidden.shape
    hidden_low = hidden.astype(jnp.bfloat16)
    projected = forward_product(hidden_low, w_proj)
    self_term = projected[:, :model_width]
    dest_term = projected[:, 2 * model_width : 3 * model_width]
    source_rows = jnp.concatenate(
        [projected[:, model_width : 2 * model_width], projected[:, 3 * model_width :]], 1
    ).astype(jnp.bfloat16)
    incoming = exchange_sources(source_rows[halo_send])
    extended = jnp.concatenate([source_rows, incoming], 0)
    edge_rows = extended[edge_src].astype(jnp.float32)
    source_b = edge_rows[:, :model_width]
    source_e = edge_rows[:, model_width:]
    edge_proj = forward_product(edge_feat, w_edge)
    gating = jax.nn.sigmoid(dest_term[edge_dst] + source_e + edge_proj)
    numerator = jax.ops.segment_sum(gating * source_b, edge_dst, row_count)
    denominator = jax.ops.segment_sum(gating, edge_dst, row_count)
    message = self_term + numerator / (denominator + GATE_EPS)
    normed_one, standard_one, inv_one = normalize(
        message, norm_gains[0], norm_shifts[0], node_total
    )
    local_out = hidden + jax.nn.silu(normed_one)
    qkv_low = forward_product(hidden_low, w_qkv).astype(jnp.bfloat16)
    query_rows = qkv_low[:, :model_width]
    key_rows = qkv_low[:, model_width : 2 * model_width]
    value_rows = qkv_low[:, 2 * model_width :]
    attn_raw, log_sum = attend_forward(query_rows, key_rows, value_rows, local_graphs, group_graphs)
    attn_low = attn_raw.reshape(row_count, model_width).astype(jnp.bfloat16)
    attn_proj = forward_product(attn_low, w_out)
    normed_two, standard_two, inv_two = normalize(
        hidden + attn_proj, norm_gains[1], norm_shifts[1], node_total
    )
    mixed = local_out + normed_two
    mixed_low = mixed.astype(jnp.bfloat16)
    up_proj = forward_product(mixed_low, w_up)
    activated = jax.nn.silu(up_proj).astype(jnp.bfloat16)
    down_proj = forward_product(activated, w_down)
    normed_three, standard_three, inv_three = normalize(
        mixed + down_proj, norm_gains[2], norm_shifts[2], node_total
    )
    saved = (
        hidden_low,
        source_b,
        gating,
        numerator,
        denominator,
        normed_one,
        standard_one,
        inv_one,
        query_rows,
        key_rows,
        value_rows,
        attn_raw,
        log_sum,
        attn_low,
        standard_two,
        inv_two,
        mixed_low,
        up_proj,
        activated,
        standard_three,
        inv_three,
    )
    return (normed_three, saved)


def layer_backward(
    grad_out,
    params,
    saved,
    edge_feat,
    edge_src,
    edge_dst,
    halo_send,
    local_graphs,
    group_graphs,
    node_total,
):
    w_proj, w_edge, w_qkv, w_out, w_up, w_down, norm_gains, norm_shifts = params
    (
        hidden_low,
        source_b,
        gating,
        numerator,
        denominator,
        normed_one,
        standard_one,
        inv_one,
        query_rows,
        key_rows,
        value_rows,
        attn_raw,
        log_sum,
        attn_low,
        standard_two,
        inv_two,
        mixed_low,
        up_proj,
        activated,
        standard_three,
        inv_three,
    ) = saved
    row_count, model_width = grad_out.shape
    grad_three, gain_three, shift_three = normalize_back(
        grad_out, standard_three, inv_three, norm_gains[2], node_total
    )
    down_grad = grad_three.astype(jnp.bfloat16)
    grad_w_down = outer_product(activated, down_grad)
    up_grad = (times_transposed(down_grad, w_down) * silu_slope_plain(up_proj)).astype(jnp.bfloat16)
    grad_w_up = outer_product(mixed_low, up_grad)
    grad_mixed = grad_three + times_transposed(up_grad, w_up)
    grad_two, gain_two, shift_two = normalize_back(
        grad_mixed, standard_two, inv_two, norm_gains[1], node_total
    )
    out_grad = grad_two.astype(jnp.bfloat16)
    grad_w_out = outer_product(attn_low, out_grad)
    attn_grad = times_transposed(out_grad, w_out).astype(jnp.bfloat16)
    grad_query, grad_key, grad_value = attend_backward(
        query_rows, key_rows, value_rows, attn_grad, attn_raw, log_sum, local_graphs, group_graphs
    )
    qkv_grad = jnp.concatenate([grad_query, grad_key, grad_value], 1).astype(jnp.bfloat16)
    grad_w_qkv = outer_product(hidden_low, qkv_grad)
    grad_message, gain_one, shift_one = normalize_back(
        grad_mixed * silu_slope_plain(normed_one), standard_one, inv_one, norm_gains[0], node_total
    )
    shifted = denominator + GATE_EPS
    grad_numer = grad_message / shifted
    grad_denom = -grad_message * numerator / (shifted * shifted)
    numer_edge = grad_numer[edge_dst]
    grad_gate = numer_edge * source_b + grad_denom[edge_dst]
    grad_pre_edge = grad_gate * gating * (1.0 - gating)
    edge_grad = grad_pre_edge.astype(jnp.bfloat16)
    grad_w_edge = outer_product(edge_feat, edge_grad)
    grad_dest = jax.ops.segment_sum(grad_pre_edge, edge_dst, row_count)
    grad_extended = jax.ops.segment_sum(
        jnp.concatenate([numer_edge * gating, grad_pre_edge], 1),
        edge_src,
        row_count + halo_send.shape[0],
    )
    returned = return_sources(grad_extended[row_count:])
    grad_source = grad_extended[:row_count].at[halo_send].add(returned)
    proj_grad = jnp.concatenate(
        [grad_message, grad_source[:, :model_width], grad_dest, grad_source[:, model_width:]], 1
    ).astype(jnp.bfloat16)
    grad_w_proj = outer_product(hidden_low, proj_grad)
    grad_hidden = (
        grad_mixed
        + grad_two
        + times_transposed(proj_grad, w_proj)
        + times_transposed(qkv_grad, w_qkv)
    )
    weight_grads = (grad_w_proj, grad_w_edge, grad_w_qkv, grad_w_out, grad_w_up, grad_w_down)
    return (
        grad_hidden,
        weight_grads,
        jnp.stack([gain_one, gain_two, gain_three]),
        jnp.stack([shift_one, shift_two, shift_three]),
    )


def per_device(
    node_input,
    edge_feat,
    graph_ids,
    edge_src,
    edge_dst,
    halo_send,
    w_proj,
    w_edge,
    w_qkv,
    w_out,
    w_up,
    w_down,
    norm_gain,
    norm_shift,
    cotangent,
):
    group_graphs = lax.all_gather(graph_ids, "nodes", axis=0, tiled=True)
    node_total = node_input.shape[0] * lax.axis_size("nodes") * lax.axis_size("rep")
    layer_count = w_proj.shape[0]
    layer_params = [
        (
            w_proj[layer_index],
            w_edge[layer_index],
            w_qkv[layer_index],
            w_out[layer_index],
            w_up[layer_index],
            w_down[layer_index],
            norm_gain[layer_index],
            norm_shift[layer_index],
        )
        for layer_index in range(layer_count)
    ]
    hidden = node_input.astype(jnp.float32)
    saved_all = []
    for layer_index in range(layer_count):
        hidden, saved = layer_forward(
            hidden,
            layer_params[layer_index],
            edge_feat,
            edge_src,
            edge_dst,
            halo_send,
            graph_ids,
            group_graphs,
            node_total,
        )
        saved_all.append(saved)
    grad_hidden = cotangent.astype(jnp.float32)
    weight_parts = [None] * layer_count
    gain_parts = [None] * layer_count
    shift_parts = [None] * layer_count
    for layer_index in range(layer_count - 1, -1, -1):
        (
            grad_hidden,
            weight_parts[layer_index],
            gain_parts[layer_index],
            shift_parts[layer_index],
        ) = layer_backward(
            grad_hidden,
            layer_params[layer_index],
            saved_all[layer_index],
            edge_feat,
            edge_src,
            edge_dst,
            halo_send,
            graph_ids,
            group_graphs,
            node_total,
        )
    proj_local = jnp.stack([weight_parts[layer_index][0] for layer_index in range(layer_count)])
    edge_local = jnp.stack([weight_parts[layer_index][1] for layer_index in range(layer_count)])
    qkv_local = jnp.stack([weight_parts[layer_index][2] for layer_index in range(layer_count)])
    out_local = jnp.stack([weight_parts[layer_index][3] for layer_index in range(layer_count)])
    up_local = jnp.stack([weight_parts[layer_index][4] for layer_index in range(layer_count)])
    down_local = jnp.stack([weight_parts[layer_index][5] for layer_index in range(layer_count)])
    grad_proj, grad_edge, grad_qkv, grad_out, grad_up, grad_down = lax.psum(
        (proj_local, edge_local, qkv_local, out_local, up_local, down_local), ("nodes", "rep")
    )
    return (
        hidden,
        grad_hidden,
        grad_proj,
        grad_edge,
        grad_qkv,
        grad_out,
        grad_up,
        grad_down,
        jnp.stack(gain_parts),
        jnp.stack(shift_parts),
    )


def solution(mesh):
    in_specs = (
        P(("rep", "nodes"), None),
        P(("rep", "nodes"), None),
        P(("rep", "nodes")),
        P(("rep", "nodes")),
        P(("rep", "nodes")),
        P(("rep", "nodes")),
        P(),
        P(),
        P(),
        P(),
        P(),
        P(),
        P(),
        P(),
        P(("rep", "nodes"), None),
    )
    out_specs = (
        P(("rep", "nodes"), None),
        P(("rep", "nodes"), None),
        P(),
        P(),
        P(),
        P(),
        P(),
        P(),
        P(),
        P(),
    )
    N, M = mesh.shape["nodes"], mesh.shape["rep"]
    fused = N in (4, 8) and M % 2 == 0 and 512 % (16 * N * M) == 0
    return jax.shard_map(
        functools.partial(fused_device, N, M) if fused else per_device,
        mesh=mesh, in_specs=in_specs, out_specs=out_specs, check_vma=False,
    )
```

```python
import functools
import math

import jax
import jax.numpy as jnp
from jax import lax
from jax.experimental import pallas as pl
from jax.experimental.pallas import tpu as pltpu
from jax.sharding import PartitionSpec as P

HEADS = 8
HEAD_DIM = 32
NEG = -1e30
NORM_EPS = 1e-05
GATE_EPS = 1e-06
F32, BF16, I32 = jnp.float32, jnp.bfloat16, jnp.int32
MESH = pl.DeviceIdType.MESH
SYNCS = 7
GROUPS = (
    ("early", 1, 0, 2560, ("core", "y", "x", "z")),
    ("conv", 1, 0, 2560, ("core", "x", "y", "z")),
    ("qkv", 1, 0, 1536, ("core", "y", "x", "z")),
    ("early", 0, 0, 2560, ("core", "x", "y", "z")),
    ("conv", 0, 0, 2560, ("core", "y", "x", "z")),
    ("qkv", 0, 0, 1536, ("core", "x", "y", "z")),
)


def dot(left, right):
    return lax.dot_general(
        left, right, (((1,), (0,)), ((), ())), preferred_element_type=F32
    )


def dot_nt(left, right):
    return lax.dot_general(
        left, right, (((1,), (1,)), ((), ())), preferred_element_type=F32
    )


def dot_tn(left, right):
    return lax.dot_general(
        left, right, (((0,), (0,)), ((), ())), preferred_element_type=F32
    )


def split(value):
    high = value.astype(BF16)
    return high, (value - high.astype(F32)).astype(BF16)


def select_rows(onehot, value):
    high, low = split(value)
    return dot(onehot, high) + dot(onehot, low)


def sigmoid(value):
    return 1.0 / (1.0 + jnp.exp(-value))


def silu_slope(value):
    logistic = sigmoid(value)
    return logistic * (1.0 + value * (1.0 - logistic))


def col_sum(value):
    return jnp.sum(value, axis=0, keepdims=True)


def pack(first, second, third, fourth):
    halves = []
    for row in (first, second, third, fourth):
        halves += [row[:, :128], row[:, 128:]]
    return jnp.concatenate(halves, 0)


def unpack(tile):
    return [
        jnp.concatenate([tile[2 * i : 2 * i + 1], tile[2 * i + 1 : 2 * i + 2]], 1)
        for i in range(4)
    ]


def combine_pair(tiles, count):
    mean = jnp.mean(tiles[:, 0:4], 0)
    off = tiles[:, 0:4] - mean
    return jnp.concatenate([mean, jnp.sum(tiles[:, 4:8] + count * off * off, 0)], 0)


def combine_last(tiles, count):
    mean = jnp.mean(tiles[:, 0:2], 0)
    off = tiles[:, 0:2] - mean
    return jnp.concatenate(
        [
            mean,
            jnp.sum(tiles[:, 2:4], 0),
            jnp.sum(tiles[:, 4:6] + count * off * off, 0),
            jnp.sum(tiles[:, 6:8] + off * tiles[:, 2:4], 0),
        ],
        0,
    )


def combine_sum(tiles, count):
    return jnp.sum(tiles, 0)


class Refs:
    pass


def axis_sizes(N, M):
    return dict(core=2, y=M // 2, x=2, z=N // 2, rep=M, nodes=N)


def scratch_list(N, M, L, R, E):
    NZ, NB, G = N // 2, N // 4, N * R
    D, FF, W, HH = 256, 512, 4 * R, HEADS // 2 * R
    dma = lambda *shape: pltpu.SemaphoreType.DMA(shape)
    vm = lambda dtype, *shape: pltpu.VMEM(shape, dtype)
    names = dict(
        gb=vm(BF16, L, N, R, D),
        xs=vm(BF16, L, N, R, D),
        meta=vm(I32, N, 8, 256),
        ef=vm(BF16, E, D),
        cot=vm(BF16, R, D),
        wp=vm(BF16, L, D, 4 * D),
        we=vm(BF16, L, D, D),
        wqkv=vm(BF16, L, D, 3 * D),
        wo=vm(BF16, L, D, D),
        wu=vm(BF16, L, D, FF),
        wd=vm(BF16, L, FF, D),
        st1=vm(F32, SYNCS, M * N, 8, 128),
        gain=vm(F32, L, 8, D),
        shift=vm(F32, L, 8, D),
        ggain=vm(F32, L, 8, D),
        gshift=vm(F32, L, 8, D),
        iv=vm(F32, L, 8, D),
        moff=vm(F32, N, 8, D),
        move=vm(F32, 8, D),
        T=vm(BF16, E, R),
        TT=vm(BF16, R, E),
        S=vm(BF16, E, 256),
        ST=vm(BF16, 256, E),
        efT=vm(BF16, D, E),
        HP=vm(BF16, 32, R),
        HN=vm(BF16, 32, R),
        A=vm(BF16, R, 64),
        bias=vm(F32, R, G),
        ce=vm(F32, L, E, D),
        xf=vm(F32, L + 1, R, D),
        xe=vm(BF16, L, 256, D),
        xeT=vm(BF16, D, 256),
        gate=vm(F32, L, E, D),
        bs=vm(BF16, L, E, D),
        num=vm(F32, L, R, D),
        den=vm(F32, L, R, D),
        z0=vm(F32, L, R, D),
        z1=vm(F32, L, R, D),
        z2=vm(F32, L, R, D),
        kk=vm(BF16, L, G, D),
        vv=vm(BF16, L, G, D),
        kT=vm(BF16, D, G),
        vT=vm(BF16, D, G),
        od=vm(F32, NB, R, D),
        md=vm(F32, NB, R, D),
        ld=vm(F32, NB, R, D),
        rb=vm(F32, L, NB, R, D),
        pst=vm(BF16, L, HEADS * R, G),
        oraw=vm(F32, L, R, D),
        ob=vm(BF16, L, R, D),
        mb=vm(BF16, L, R, D),
        u=vm(F32, L, R, FF),
        g=vm(BF16, L, R, FF),
        dy=vm(F32, R, D),
        dmix=vm(F32, R, D),
        dxo=vm(F32, R, D),
        dob=vm(F32, R, D),
        dq=vm(F32, R, D),
        qm=vm(BF16, L, 2, HH, 128),
        qmT=vm(BF16, 2, 128, HH),
        dom=vm(BF16, HH, 128),
        dss=vm(BF16, HH, W),
        dkv=vm(BF16, 2 * D, W),
        gkv=vm(F32, 2 * D, D),
        dce=vm(BF16, E, D),
        dproj=vm(BF16, 4, 256, D),
        dxs=vm(BF16, L, NZ, 2, R, D),
        rs1=vm(BF16, L, NZ, R, D),
        cs=vm(BF16, L, NZ, R, D),
        rs2=vm(BF16, L, NZ, R, D),
        hs=vm(BF16, L, 2, 32, D),
        hr=vm(BF16, L, 2, 32, D),
    )
    names.update(
        load=dma(10),
        store=dma(2),
        meta_s=dma(1),
        meta_r=dma(1),
        st1_s=dma(SYNCS),
        st1_r=dma(SYNCS),
        agc_s=dma(L, NZ),
        agc_r=dma(L, NZ),
        agp_s=dma(L, NZ),
        agp_r=dma(L, NZ),
        rsp_s=dma(L, NZ),
        rsp_r=dma(L, NZ),
        rsc_s=dma(L, NZ),
        rsc_r=dma(L, NZ),
        hal_s=dma(L, 2),
        hal_r=dma(L, 2),
    )
    return names


IN_NAMES = (
    "x_in", "ids", "edge_src", "edge_dst", "halo", "ef_h", "wp_h", "we_h", "wqkv_h", "wo_h", "wu_h", "wd_h",
    "gain_in", "shift_in", "cot_h",
)
OUT_NAMES = ("out_act", "grad_in", "gs_early", "gs_conv", "gs_qkv", "ggain_out", "gshift_out")


def kernel(N, M, L, names, *args):
    r_ = Refs()
    for name, ref in zip(IN_NAMES + OUT_NAMES + tuple(names), args, strict=True):
        setattr(r_, name, ref)
    R, D = r_.x_in.shape
    E = r_.ef.shape[0]
    NZ, NB, G, W = N // 2, N // 4, N * R, 4 * R
    HK = HEADS // 2
    total = float(N * M * R)
    scale = HEAD_DIM ** -0.5
    me = lax.axis_index("nodes")
    rep = lax.axis_index("rep")
    z = me // 2
    par = me % 2
    partner = 2 * z + (1 - par)
    prev = (me + N - 1) % N
    nxt = (me + 1) % N
    zh, zl = z // 2, z % 2
    z_to = lambda t: 2 * ((zh + t // 2) % NB) + (zl + t % 2) % 2
    z_from = lambda t: 2 * ((zh + NB - t // 2) % NB) + (zl + t % 2) % 2

    def remote(src, dst, s_sem, r_sem, **where):
        return pltpu.make_async_remote_copy(
            src_ref=src, dst_ref=dst, send_sem=s_sem, recv_sem=r_sem,
            device_id=where, device_id_type=MESH,
        )

    def send(src, dst, s_sem, r_sem, **where):
        remote(src, dst, s_sem, r_sem, **where).start()

    def arrive(dst, r_sem):
        remote(dst, dst, r_sem, r_sem, nodes=partner).wait_recv()

    def sent(src, s_sem):
        remote(src, src, s_sem, s_sem, nodes=partner).wait_send()

    def when(condition, *acts):
        @pl.when(condition)
        def _():
            for act in acts:
                act()

    loads = [
        pltpu.make_async_copy(getattr(r_, f"{name}_h"), getattr(r_, name), r_.load.at[i])
        for i, name in enumerate(("ef", "we", "wqkv", "wp", "wo", "wu", "wd", "cot"))
    ]
    own_rows = pltpu.make_async_copy(r_.x_in, r_.gb.at[0, me], r_.load.at[8])
    own_rows.start()
    for load in loads:
        load.start()

    barrier = pltpu.get_barrier_semaphore()
    for dr in range(M):
        for d in range(N):
            if dr + d > 0:
                pl.semaphore_signal(barrier, inc=1, device_id={"rep": (rep + dr) % M, "nodes": (me + d) % N},
                                    device_id_type=MESH)
    pl.semaphore_wait(barrier, M * N - 1)

    def gather_start(l):
        mine = r_.gb.at[l, me]
        send(mine, mine, r_.agp_s.at[l, 0], r_.agp_r.at[l, 0], nodes=partner)
        for t in range(1, NZ):
            send(mine, mine, r_.agc_s.at[l, t], r_.agc_r.at[l, t], nodes=2 * z_to(t) + par)

    def gather_pass(l, t):
        piece = r_.gb.at[l, 2 * z_from(t) + par]
        arrive(piece, r_.agc_r.at[l, t])
        send(piece, piece, r_.agp_s.at[l, t], r_.agp_r.at[l, t], nodes=partner)

    def gather_take(l, t):
        arrive(r_.gb.at[l, 2 * z_from(t) + 1 - par], r_.agp_r.at[l, t])

    def sync_start(k, tile):
        mine = rep * N + me
        r_.st1[k, mine] = tile
        for dr in range(M):
            for d in range(N):
                if dr + d > 0:
                    send(r_.st1.at[k, mine], r_.st1.at[k, mine], r_.st1_s.at[k], r_.st1_r.at[k],
                         rep=(rep + dr) % M, nodes=(me + d) % N)

    def sync_finish(k, combine):
        arrive(r_.st1.at[k, 0 : M * N - 1], r_.st1_r.at[k])
        return unpack(combine(r_.st1[k], float(R)))

    def put(buf, l, at, value):
        rows = value.shape[0]
        for c in range(value.shape[1] // 128):
            buf[l, at : at + rows] = value[:, 128 * c : 128 * (c + 1)].astype(BF16)
            at += rows
        return at

    lane_head = lax.broadcasted_iota(I32, (R, 128), 1) // HEAD_DIM

    def by_head(parts):
        out = parts[0]
        for k in range(1, HK):
            out = jnp.where(lane_head == k, parts[k], out)
        return out

    r_.meta[me] = jnp.full((8, 256), -1, I32)
    r_.meta[me, 0:1, 0:R] = r_.ids[...].reshape(1, R)
    r_.meta[me, 1:2, 0:48] = r_.halo[...].reshape(1, 48)
    for d in range(1, N):
        send(r_.meta.at[me], r_.meta.at[me], r_.meta_s.at[0], r_.meta_r.at[0], nodes=(me + d) % N)
    own_rows.wait()
    gather_start(0)

    src_row = r_.edge_src[...].reshape(1, E)
    src_row = jnp.where(src_row < R + 24, src_row, src_row + 8)
    dst_row = r_.edge_dst[...].reshape(1, E)
    src_col = jnp.broadcast_to(src_row, (128, E)).T[:, 0:1]
    dst_col = jnp.broadcast_to(dst_row, (128, E)).T[:, 0:1]
    as_mask = lambda cond: cond.astype(F32).astype(BF16)
    r_.T[...] = as_mask(dst_col == lax.broadcasted_iota(I32, (E, R), 1))
    r_.TT[...] = as_mask(dst_row == lax.broadcasted_iota(I32, (R, E), 0))
    r_.S[...] = as_mask(src_col == lax.broadcasted_iota(I32, (E, 256), 1))
    r_.ST[...] = as_mask(src_row == lax.broadcasted_iota(I32, (256, E), 0))
    loads[0].wait()
    r_.efT[...] = r_.ef[...].T
    loads[1].wait()
    for l in range(L):
        r_.ce[l] = dot(r_.ef[...], r_.we[l])
        for k in range(3):
            r_.gain[l, k : k + 1] = r_.gain_in[k, l : l + 1]
            r_.shift[l, k : k + 1] = r_.shift_in[k, l : l + 1]
    r_.xf[0] = r_.gb[0, me].astype(F32)
    r_.moff[...] = jnp.zeros((N, 8, D), F32)
    r_.move[0:1] = jnp.ones((1, D), F32)
    r_.move[1:2] = jnp.zeros((1, D), F32)
    for load in loads[2:]:
        load.wait()

    arrive(r_.meta.at[0 : N - 1], r_.meta_r.at[0])
    id_col = jnp.broadcast_to(r_.meta[me][0:1, 0:R], (128, R)).T[:, 0:1]
    id_row = jnp.concatenate([r_.meta[j][0:1, 0:R] for j in range(N)], 1)
    r_.bias[...] = jnp.where(id_col == id_row, 0.0, NEG)

    def halo_onehot(device, start):
        col = jnp.broadcast_to(r_.meta[device][1:2, 0:128], (128, 128)).T[start : start + 24, 0:1]
        hot = (col == lax.broadcasted_iota(I32, (24, R), 1)).astype(F32)
        return jnp.concatenate([hot, jnp.zeros((8, R), F32)], 0).astype(BF16)

    r_.HP[...] = halo_onehot(prev, 24)
    r_.HN[...] = halo_onehot(nxt, 0)
    r_.A[...] = as_mask(r_.meta[me][1:2, 0:64] == lax.broadcasted_iota(I32, (R, 64), 0))

    factor_exp = scale * math.log2(math.e)

    def prepare_queries(l):
        q = dot(r_.xs[l, me], r_.wqkv[l, :, :D]).astype(BF16).astype(F32)
        for hf in range(2):
            for k in range(HK):
                part = jnp.where(lane_head == k, q[:, 128 * hf : 128 * (hf + 1)], 0.0)
                r_.qm[l, hf, k * R : (k + 1) * R] = part.astype(BF16)

    def head_rows(hf, k, count=1):
        return pl.ds(pl.multiple_of((hf * HK + k) * R, 64), count * R)

    def lane_half(hf):
        return pl.ds(pl.multiple_of(hf * 128, 128), 128)

    def attention_block(l, i, middle):
        half = (zh + NB - i) % NB
        rows = pl.ds(pl.multiple_of(half * W, 128), W)
        x = r_.xs[l, pl.ds(4 * half, 4)].reshape(W, D)
        key = dot(x, r_.wqkv[l, :, D : 2 * D]).astype(BF16)
        r_.kk[l, rows] = key
        r_.kT[:, rows] = key.T
        r_.vv[l, rows] = dot(x, r_.wqkv[l, :, 2 * D :]).astype(BF16)

        def heads(hf, carry):
            lanes = lane_half(hf)
            tops, sums, outs = [], [], []
            for c in range(HK // 2):
                scores = dot(r_.qm[l, hf, 2 * c * R : 2 * (c + 1) * R], r_.kT[lanes, rows])
                for k in range(2):
                    s = scores[k * R : (k + 1) * R] + r_.bias[:, rows]
                    top = jnp.max(s, 1, keepdims=True)
                    e = jnp.exp2((s - top) * factor_exp)
                    tops.append(top)
                    sums.append(jnp.sum(e, 1, keepdims=True))
                    r_.pst[l, head_rows(hf, 2 * c + k), rows] = e.astype(BF16)
                o = dot(r_.pst[l, head_rows(hf, 2 * c, 2), rows], r_.vv[l, rows, lanes])
                outs += [o[0:R], o[R : 2 * R]]
            r_.md[i, :, lanes] = by_head([jnp.broadcast_to(v, (R, 128)) for v in tops])
            r_.ld[i, :, lanes] = by_head([jnp.broadcast_to(v, (R, 128)) for v in sums])
            r_.od[i, :, lanes] = by_head(outs)
            middle(i, hf)
            return carry

        lax.fori_loop(0, 2, heads, 0)

    def attention_end(l):
        top = r_.md[0]
        for i in range(1, NB):
            top = jnp.maximum(top, r_.md[i])
        factors = [jnp.exp2((r_.md[i] - top) * factor_exp) for i in range(NB)]
        inv = 1.0 / sum(factors[i] * r_.ld[i] for i in range(NB))
        o = jnp.zeros((R, D), F32)
        for i in range(NB):
            r_.rb[l, i] = factors[i] * inv
            o = o + factors[i] * inv * r_.od[i]
        r_.oraw[l] = o
        ob = o.astype(BF16)
        r_.ob[l] = ob
        t1 = r_.xf[l] + dot(ob, r_.wo[l])
        r_.z1[l] = t1
        mean1 = col_sum(t1) / R
        return mean1, col_sum((t1 - mean1) * (t1 - mean1))

    def convolution(l):
        xs = r_.xs
        xb = xs[l, me]
        r_.xe[l, 0:R] = xb
        r_.xe[l, R : R + 32] = dot(r_.HP[...], xs[l, prev]).astype(BF16)
        r_.xe[l, R + 32 : R + 64] = dot(r_.HN[...], xs[l, nxt]).astype(BF16)
        xe = r_.xe[l]
        tab_b = dot(xe, r_.wp[l, :, D : 2 * D]).astype(BF16)
        tab_e = dot(xe, r_.wp[l, :, 3 * D :]).astype(BF16)
        pa = dot(xb, r_.wp[l, :, 0:D])
        pd = dot(xb, r_.wp[l, :, 2 * D : 3 * D])
        bs = dot(r_.S[...], tab_b)
        r_.bs[l] = bs.astype(BF16)
        gate = sigmoid(select_rows(r_.T[...], pd) + dot(r_.S[...], tab_e) + r_.ce[l])
        r_.gate[l] = gate
        num = select_rows(r_.TT[...], gate * bs)
        den = select_rows(r_.TT[...], gate)
        r_.num[l] = num
        r_.den[l] = den
        msg = pa + num / (den + GATE_EPS)
        r_.z0[l] = msg

    def forward(l, carry):
        def ready(js):
            for j in js:
                moved = (r_.gb[l, j].astype(F32) + r_.moff[j, 0:1]) * r_.move[0:1] + r_.move[1:2]
                r_.xs[l, j] = moved.astype(BF16)

        r_.xs[l, me] = r_.xf[l].astype(BF16)
        gather_pass(l, 1)
        prepare_queries(l)
        gather_take(l, 0)
        gather_take(l, 1)
        ready([partner, 2 * z_from(1) + par, 2 * z_from(1) + 1 - par])

        def middle(i, hf):
            for t in range(2, NZ):
                when((i == 0) & (hf == t - 2), lambda: gather_pass(l, t))

        def block(i, carry):
            attention_block(l, i, middle)

            @pl.when(i == 0)
            def _():
                for t in range(2, NZ):
                    gather_take(l, t)
                ready([2 * z_from(t) + p for t in range(2, NZ) for p in range(2)])
                convolution(l)

            return carry

        lax.fori_loop(0, NB, block, 0)
        mean1, sq1 = attention_end(l)
        msg = r_.z0[l]
        mean0 = col_sum(msg) / R
        sq0 = col_sum((msg - mean0) * (msg - mean0))
        sync_start(2 * l, pack(mean0, mean1, sq0, sq1))
        mean0, mean1, sq0, sq1 = sync_finish(2 * l, combine_pair)
        inv0 = lax.rsqrt(sq0 / total + NORM_EPS)
        inv1 = lax.rsqrt(sq1 / total + NORM_EPS)
        r_.iv[l, 0:1] = inv0
        r_.iv[l, 1:2] = inv1
        z0 = (r_.z0[l] - mean0) * inv0
        z1 = (r_.z1[l] - mean1) * inv1
        r_.z0[l] = z0
        r_.z1[l] = z1
        n0 = z0 * r_.gain[l, 0:1] + r_.shift[l, 0:1]
        mix = r_.xf[l] + n0 * sigmoid(n0) + z1 * r_.gain[l, 1:2] + r_.shift[l, 1:2]
        mb = mix.astype(BF16)
        r_.mb[l] = mb
        u = dot(mb, r_.wu[l])
        r_.u[l] = u
        g = (u * sigmoid(u)).astype(BF16)
        r_.g[l] = g
        y = mix + dot(g, r_.wd[l])
        r_.z2[l] = y
        mean = col_sum(y) / R
        cent = y - mean
        k = 2 * l + 1
        dy = r_.cot[...].astype(F32)
        sync_start(k, pack(mean, col_sum(dy), col_sum(cent * cent), col_sum(dy * cent)))

        @pl.when(l < L - 1)
        def _():
            r_.gb[l + 1, me] = cent.astype(BF16)
            gather_start(l + 1)

        tot_mean, dy_sum, tot_sq, dy_cent = sync_finish(k, combine_last)
        inv2 = lax.rsqrt(tot_sq / total + NORM_EPS)
        r_.iv[l, 2:3] = inv2
        z2 = (r_.z2[l] - tot_mean) * inv2
        r_.z2[l] = z2
        gain, shift = r_.gain[l, 2:3], r_.shift[l, 2:3]
        r_.xf[l + 1] = z2 * gain + shift
        r_.gshift[l, 2:3] = dy_sum
        r_.ggain[l, 2:3] = dy_cent * inv2
        for j in range(N):
            tile = r_.st1[k, rep * N + j]
            r_.moff[j, 0:1] = jnp.concatenate([tile[0:1], tile[1:2]], 1) - tot_mean
        r_.move[0:1] = inv2 * gain
        r_.move[1:2] = shift
        return carry

    lax.fori_loop(0, L, forward, 0)
    act_copy = pltpu.make_async_copy(r_.xf.at[L], r_.out_act, r_.store.at[0])
    act_copy.start()

    def back_feed_forward(l, k):
        s2, g2 = r_.gshift[l, 2:3], r_.ggain[l, 2:3]
        d3 = r_.gain[l, 2:3] * r_.iv[l, 2:3] * (r_.dy[...] - s2 / total - r_.z2[l] * (g2 / total))
        db = d3.astype(BF16)
        dub = (dot_nt(db, r_.wd[l]) * silu_slope(r_.u[l])).astype(BF16)
        dmix = d3 + dot_nt(dub, r_.wu[l])
        r_.dmix[...] = dmix
        n0 = r_.z0[l] * r_.gain[l, 0:1] + r_.shift[l, 0:1]
        gy0 = dmix * silu_slope(n0)
        sync_start(k, pack(col_sum(dmix), col_sum(dmix * r_.z1[l]), col_sum(gy0), col_sum(gy0 * r_.z0[l])))
        at = put(r_.gs_early, l, 512, dot_tn(r_.mb[l], dub))
        put(r_.gs_early, l, at, dot_tn(r_.g[l], db))
        r_.vT[...] = r_.vv[l].T
        r_.xeT[...] = r_.xe[l].T
        for hf in range(2):
            r_.qmT[hf] = r_.qm[l, hf].T

    def back_norms(l, k):
        s1, g1, s0, g0 = sync_finish(k, combine_sum)
        r_.gshift[l, 1:2] = s1
        r_.ggain[l, 1:2] = g1
        r_.gshift[l, 0:1] = s0
        r_.ggain[l, 0:1] = g0
        dmix = r_.dmix[...]
        d2 = r_.gain[l, 1:2] * r_.iv[l, 1:2] * (dmix - s1 / total - r_.z1[l] * (g1 / total))
        dab = d2.astype(BF16)
        r_.dxo[...] = dmix + d2
        r_.dob[...] = dot_nt(dab, r_.wo[l]).astype(BF16).astype(F32)
        put(r_.gs_early, l, 0, dot_tn(r_.ob[l], dab))
        r_.gkv[...] = jnp.zeros((2 * D, D), F32)
        r_.dq[...] = jnp.zeros((R, D), F32)

    def back_attention_block(l, i, between):
        t1 = (i + 1) % NB
        half = (zh + t1) % NB
        rows = pl.ds(pl.multiple_of(half * W, 128), W)

        def heads(hf, carry):
            lanes = lane_half(hf)
            dos = r_.dob[:, lanes] * r_.rb[l, (NB - t1) % NB, :, lanes]
            prod = dos * r_.oraw[l, :, lanes]
            for k in range(HK):
                r_.dom[k * R : (k + 1) * R] = jnp.where(lane_head == k, dos, 0.0).astype(BF16)
            parts = []
            for c in range(HK // 2):
                both = slice(2 * c * R, 2 * (c + 1) * R)
                dp = dot(r_.dom[both], r_.vT[lanes, rows])
                for k in range(2):
                    h = 2 * c + k
                    delta = jnp.sum(jnp.where(lane_head == h, prod, 0.0), 1, keepdims=True)
                    ds = r_.pst[l, head_rows(hf, h), rows].astype(F32) * (dp[k * R : (k + 1) * R] - delta)
                    r_.dss[h * R : (h + 1) * R] = ds.astype(BF16)
                part = dot(r_.dss[both], r_.kk[l, rows, lanes])
                parts += [part[0:R], part[R : 2 * R]]
            r_.dq[:, lanes] += by_head(parts)
            dk = dot(r_.qmT[hf], r_.dss[...]) * scale
            r_.dkv[pl.ds(pl.multiple_of(hf * 128, 128), 128)] = dk.astype(BF16)
            dv = dot(r_.dom[...].T, r_.pst[l, head_rows(hf, 0, HK), rows])
            r_.dkv[pl.ds(pl.multiple_of(D + hf * 128, 128), 128)] = dv.astype(BF16)
            between(i, hf)
            return carry

        lax.fori_loop(0, 2, heads, 0)
        dx = dot(r_.wqkv[l, :, D:], r_.dkv[...]).T
        r_.dxs[l, pl.ds(2 * half, 2)] = dx.astype(BF16).reshape(2, 2, R, D)
        for low in range(2):
            zb = 2 * half + low
            send(r_.dxs.at[l, zb, 1 - par], r_.rs1.at[l, zb],
                 r_.rsp_s.at[l, 2 * i + low], r_.rsp_r.at[l, 2 * i + low], nodes=partner)
        r_.gkv[...] += dot(r_.dkv[...], r_.xs[l, pl.ds(4 * half, 4)].reshape(W, D))

    def pass_on(l, i, t):
        zb = z_to(t)
        arrive(r_.rs1.at[l, zb], r_.rsp_r.at[l, 2 * i + zb % 2])
        both = r_.dxs[l, zb, par].astype(F32) + r_.rs1[l, zb].astype(F32)
        r_.cs[l, zb] = both.astype(BF16)
        send(r_.cs.at[l, zb], r_.rs2.at[l, z], r_.rsc_s.at[l, t], r_.rsc_r.at[l, t], nodes=2 * zb + par)

    def back_convolution(l):
        s0, g0 = r_.gshift[l, 0:1], r_.ggain[l, 0:1]
        inv_den = 1.0 / (r_.den[l] + GATE_EPS)
        n0 = r_.z0[l] * r_.gain[l, 0:1] + r_.shift[l, 0:1]
        gy0 = r_.dmix[...] * silu_slope(n0)
        dm = r_.gain[l, 0:1] * r_.iv[l, 0:1] * (gy0 - s0 / total - r_.z0[l] * (g0 / total))
        dnum = dm * inv_den
        dden = -dnum * r_.num[l] * inv_den
        dnum_e = select_rows(r_.T[...], dnum)
        dden_e = select_rows(r_.T[...], dden)
        gate = r_.gate[l]
        dgp = (dnum_e * r_.bs[l].astype(F32) + dden_e) * gate * (1.0 - gate)
        r_.dce[...] = dgp.astype(BF16)
        dpb = select_rows(r_.ST[...], dnum_e * gate).astype(BF16)
        dpe = select_rows(r_.ST[...], dgp).astype(BF16)
        dpd = select_rows(r_.TT[...], dgp).astype(BF16)
        dmb = dm.astype(BF16)
        dxe = dot_nt(dpb, r_.wp[l, :, D : 2 * D]) + dot_nt(dpe, r_.wp[l, :, 3 * D :])
        r_.hs[l, 0] = dxe[R : R + 32].astype(BF16)
        r_.hs[l, 1] = dxe[R + 32 : R + 64].astype(BF16)
        send(r_.hs.at[l, 0], r_.hr.at[l, 1], r_.hal_s.at[l, 0], r_.hal_r.at[l, 0], nodes=prev)
        send(r_.hs.at[l, 1], r_.hr.at[l, 0], r_.hal_s.at[l, 1], r_.hal_r.at[l, 1], nodes=nxt)
        r_.dxo[...] += (
            dxe[0:R]
            + dot_nt(dmb, r_.wp[l, :, 0:D])
            + dot_nt(dpd, r_.wp[l, :, 2 * D : 3 * D])
        )
        r_.dproj[0, 0:R] = dmb
        r_.dproj[1] = dpb
        r_.dproj[2, 0:R] = dpd
        r_.dproj[3] = dpe
        at = 0
        for c in range(4):
            width = R if c % 2 == 0 else 256
            at = put(r_.gs_conv, l, at, dot(r_.xeT[:, 0:width], r_.dproj[c, 0:width]))
        put(r_.gs_conv, l, at, dot(r_.efT[...], r_.dce[...]))

    def back_input(l):
        dx = r_.dxo[...]
        arrive(r_.rs1.at[l, z], r_.rsp_r.at[l, 2 * (NB - 1) + zl])
        dx = dx + r_.dxs[l, z, par].astype(F32) + r_.rs1[l, z].astype(F32)
        for t in range(1, NZ):
            c = z_from(t)
            arrive(r_.rs2.at[l, c], r_.rsc_r.at[l, t])
            dx = dx + r_.rs2[l, c].astype(F32)
        arrive(r_.hr.at[l, 0], r_.hal_r.at[l, 1])
        arrive(r_.hr.at[l, 1], r_.hal_r.at[l, 0])
        back = jnp.concatenate(
            [r_.hr[l, 0].astype(F32)[0:24], r_.hr[l, 1].astype(F32)[0:24], jnp.zeros((16, D), F32)], 0
        )
        return dx + dot(r_.A[...], back.astype(BF16))

    r_.dy[...] = r_.cot[...].astype(F32)

    def backward(b, carry):
        l = L - 1 - b
        first = b == 0
        k = 4 + 2 * b
        back_feed_forward(l, k)
        back_norms(l, k)

        def between(i, hf):
            for t in range(2, NZ):
                when((i == 1) & (hf == 0), functools.partial(pass_on, l, 0, t))

        def block(i, carry):
            back_attention_block(l, i, between)

            @pl.when(i == 0)
            def _():
                back_convolution(l)

            return carry

        lax.fori_loop(0, NB, block, 0)
        dqb = (r_.dq[...] * scale).astype(BF16)
        at = put(r_.gs_qkv, l, 0, dot(r_.xeT[:, 0:R], dqb))
        put(r_.gs_qkv, l, at, r_.gkv[...].T)
        r_.dxo[...] += dot_nt(dqb, r_.wqkv[l, :, 0:D])
        pass_on(l, NB - 1, 1)
        dx = back_input(l)
        r_.dy[...] = dx

        @pl.when(first)
        def _():
            below = L - 2
            zero_row = jnp.zeros((1, D), F32)
            sync_start(5, pack(col_sum(dx), col_sum(dx * r_.z2[below]), zero_row, zero_row))
            s2, g2, _, _ = sync_finish(5, combine_sum)
            r_.gshift[below, 2:3] = s2
            r_.ggain[below, 2:3] = g2

        return carry

    lax.fori_loop(0, L, backward, 0)
    in_copy = pltpu.make_async_copy(r_.dy, r_.grad_in, r_.store.at[1])
    in_copy.start()
    for l in range(L):
        for k in range(3):
            r_.ggain_out[k, l : l + 1] = r_.ggain[l, k : k + 1]
            r_.gshift_out[k, l : l + 1] = r_.gshift[l, k : k + 1]
    sent(r_.meta.at[0 : N - 1], r_.meta_s.at[0])
    for k in range(SYNCS):
        sent(r_.st1.at[k, 0 : M * N - 1], r_.st1_s.at[k])
    for l in range(L):
        for t in range(NZ):
            sent(r_.gb.at[l, 0], r_.agp_s.at[l, t])
            sent(r_.rs1.at[l, 0], r_.rsp_s.at[l, t])
            if t > 0:
                sent(r_.gb.at[l, 0], r_.agc_s.at[l, t])
                sent(r_.rs1.at[l, 0], r_.rsc_s.at[l, t])
        for side in range(2):
            sent(r_.hs.at[l, 0], r_.hal_s.at[l, side])
    act_copy.wait()
    in_copy.wait()


def reduce_scratch(N, M):
    dma = lambda *shape: pltpu.SemaphoreType.DMA(shape)
    vm = lambda dtype, *shape: pltpu.VMEM(shape, dtype)
    names = dict(
        gs_early=vm(BF16, 2, 2560, 128),
        gs_conv=vm(BF16, 2, 2560, 128),
        gs_qkv=vm(BF16, 2, 1536, 128),
    )
    sizes = axis_sizes(N, M)
    for g, (_, _, _, rows, stages) in enumerate(GROUPS):
        names[f"go{g}"] = vm(BF16, rows, 128)
        left = rows
        for k, axis in enumerate(stages):
            left //= sizes[axis]
            names[f"ga{g}_{k}"] = vm(BF16, sizes[axis] - 1, left, 128)
            if k < len(stages) - 1:
                names[f"gh{g}_{k}"] = vm(BF16, left, 128)
    names.update(load=dma(3), ar_s=dma(len(GROUPS), 8), ar_r=dma(len(GROUPS), 8), ar_l=dma(len(GROUPS)))
    return names


def reduce_kernel(N, M, names, *args):
    r_ = Refs()
    outs = tuple(f"gout{g}" for g in range(len(GROUPS)))
    for name, ref in zip(("early_h", "conv_h", "qkv_h") + outs + tuple(names), args, strict=True):
        setattr(r_, name, ref)
    me = lax.axis_index("nodes")
    rep = lax.axis_index("rep")
    z = me // 2
    par = me % 2
    partner = 2 * z + (1 - par)
    loads = [
        pltpu.make_async_copy(getattr(r_, f"{name}_h"), getattr(r_, f"gs_{name}"), r_.load.at[i])
        for i, name in enumerate(("early", "conv", "qkv"))
    ]
    for load in loads:
        load.start()

    def remote(src, dst, s_sem, r_sem, **where):
        return pltpu.make_async_remote_copy(
            src_ref=src, dst_ref=dst, send_sem=s_sem, recv_sem=r_sem,
            device_id=where, device_id_type=MESH,
        )

    def send(src, dst, s_sem, r_sem, **where):
        remote(src, dst, s_sem, r_sem, **where).start()

    def arrive(dst, r_sem):
        remote(dst, dst, r_sem, r_sem, nodes=partner).wait_recv()

    def sent(src, s_sem):
        remote(src, src, s_sem, s_sem, nodes=partner).wait_send()

    barrier = pltpu.get_barrier_semaphore()
    for d in range(1, N):
        pl.semaphore_signal(barrier, inc=1, device_id={"nodes": (me + d) % N}, device_id_type=MESH)
    for d in range(1, M):
        pl.semaphore_signal(barrier, inc=1, device_id={"rep": (rep + d) % M}, device_id_type=MESH)
    pl.semaphore_wait(barrier, N + M - 2)
    for load in loads:
        load.wait()

    sizes = axis_sizes(N, M)
    core, row = rep % 2, rep // 2
    places = dict(
        core=(core, lambda t: dict(rep=2 * row + t)),
        y=(row, lambda t: dict(rep=2 * t + core)),
        x=(par, lambda t: dict(nodes=2 * z + t)),
        z=(z, lambda t: dict(nodes=2 * t + par)),
        rep=(rep, lambda t: dict(rep=t)),
        nodes=(me, lambda t: dict(nodes=t)),
    )

    def reduce_step(g, step):
        name, layer, first, rows, stages = GROUPS[g]
        K = len(stages)
        gs, out = getattr(r_, f"gs_{name}").at[layer, first : first + rows], getattr(r_, f"go{g}")
        count, offset = [rows], [0]
        for axis in stages:
            count.append(count[-1] // sizes[axis])
            offset.append(offset[-1] + places[axis][0] * count[-1])
        take = lambda start, size: pl.ds(pl.multiple_of(start, 16), size)
        if 1 <= step <= K:
            k = step - 1
            got = getattr(r_, f"ga{g}_{k}")
            arrive(got, r_.ar_r.at[g, k])
            held = gs if k == 0 else getattr(r_, f"gh{g}_{k - 1}")
            index = places[stages[k]][0]
            acc = held[take(index * count[k + 1], count[k + 1])].astype(F32)
            for slot in range(sizes[stages[k]] - 1):
                acc = acc + got[slot].astype(F32)
            if step < K:
                getattr(r_, f"gh{g}_{k}")[...] = acc.astype(BF16)
            else:
                out[take(offset[K], count[K])] = acc.astype(BF16)
        elif step > K:
            k = 2 * K - step
            arrive(out.at[0 : (sizes[stages[k]] - 1) * count[k + 1]], r_.ar_r.at[g, step - 1])
        if step < K:
            held = gs if step == 0 else getattr(r_, f"gh{g}_{step - 1}")
            index, device = places[stages[step]]
            size = sizes[stages[step]]
            for d in range(1, size):
                to = (index + d) % size
                send(held.at[take(to * count[step + 1], count[step + 1])], getattr(r_, f"ga{g}_{step}").at[d - 1],
                     r_.ar_s.at[g, step], r_.ar_r.at[g, step], **device(to))
        elif step < 2 * K:
            k = 2 * K - 1 - step
            index, device = places[stages[k]]
            size = sizes[stages[k]]
            here = out.at[take(offset[k + 1], count[k + 1])]
            for d in range(1, size):
                send(here, here, r_.ar_s.at[g, step], r_.ar_r.at[g, step], **device((index + d) % size))
        else:
            pltpu.make_async_copy(out, getattr(r_, f"gout{g}"), r_.ar_l.at[g]).start()

    def reduce_drain(g):
        _, _, _, rows, stages = GROUPS[g]
        K, left = len(stages), rows
        out = getattr(r_, f"go{g}")
        for k, axis in enumerate(stages):
            left //= sizes[axis]
            for step in (k, 2 * K - 1 - k):
                sent(out.at[0 : (sizes[axis] - 1) * left], r_.ar_s.at[g, step])
        pltpu.make_async_copy(out, getattr(r_, f"gout{g}"), r_.ar_l.at[g]).wait()

    for slot in range(2 * 4 + 1 + 2):
        for g in range(len(GROUPS)):
            if 0 <= slot - g // 2 <= 2 * 4:
                reduce_step(g, slot - g // 2)
    for g in range(len(GROUPS)):
        reduce_drain(g)


def finish_kernel(act_h, gin_h, *refs):
    n = len(GROUPS)
    held, (ggain_h, gshift_h), refs = refs[:n], refs[n : n + 2], refs[n + 2 :]
    act_o, gin_o, proj_o, edge_o, qkv_o, out_o, up_o, down_o, ggain_o, gshift_o = refs[:10]
    summed, refs = refs[10 : 10 + n], refs[10 + n :]
    act, gin, proj, edge, qkv, out, up, down, in_sem, out_sem = refs
    loads = [
        pltpu.make_async_copy(src, dst, in_sem.at[i])
        for i, (src, dst) in enumerate(zip(held + (act_h, gin_h), summed + (act, gin), strict=True))
    ]
    for load in loads:
        load.start()
    ggain_o[...] = ggain_h[...]
    gshift_o[...] = gshift_h[...]
    stores = []

    def store(src, dst):
        copy = pltpu.make_async_copy(src, dst, out_sem.at[len(stores)])
        copy.start()
        stores.append(copy)

    def widen(dst, l, g, at, first=0, last=None):
        rows = dst.shape[1]
        for c in range(first, dst.shape[2] // 128 if last is None else last):
            dst[l, :, 128 * c : 128 * (c + 1)] = summed[g][at : at + rows].astype(F32)
            at += rows
        return at

    for g, (name, l, first, rows, _) in enumerate(GROUPS):
        loads[g].wait()
        if name == "early":
            at = widen(out, l, g, 0)
            store(out.at[l], out_o.at[l])
            at = widen(up, l, g, at)
            store(up.at[l], up_o.at[l])
            widen(down, l, g, at)
            store(down.at[l], down_o.at[l])
        elif name == "conv":
            at = widen(proj, l, g, 0)
            store(proj.at[l], proj_o.at[l])
            widen(edge, l, g, at)
            store(edge.at[l], edge_o.at[l])
        else:
            widen(qkv, l, g, 0, first // 256, (first + rows) // 256)
            if first + rows == 1536:
                store(qkv.at[l], qkv_o.at[l])
    for i, (src, dst) in enumerate(((act, act_o), (gin, gin_o))):
        loads[n + i].wait()
        store(src, dst)
    for copy in stores:
        copy.wait()


def fused_device(
    N, M, node_input, edge_feat, graph_ids, edge_src, edge_dst, halo_send, w_proj, w_edge, w_qkv,
    w_out, w_up, w_down, norm_gain, norm_shift, cotangent,
):
    R, D = node_input.shape
    E = edge_feat.shape[0]
    L = w_proj.shape[0]
    names = scratch_list(N, M, L, R, E)
    vmem = pl.BlockSpec(memory_space=pltpu.VMEM)
    hbm = pl.BlockSpec(memory_space=pltpu.HBM)
    shape = jax.ShapeDtypeStruct
    rows = shape((R, D), F32)
    norm = shape((3, L, D), F32)
    groups = [shape((rows_g, 128), BF16) for _, _, _, rows_g, _ in GROUPS]
    partial = [shape((L, count, 128), BF16) for count in (2560, 2560, 1536)]
    act, gin, early, conv, qkv, ggain, gshift = pl.pallas_call(
        functools.partial(kernel, N, M, L, tuple(names)),
        out_shape=[rows, rows, *partial, norm, norm],
        in_specs=[hbm] + [vmem] * 4 + [hbm] * 7 + [vmem] * 2 + [hbm],
        out_specs=[hbm] * 2 + [vmem] * 5,
        scratch_shapes=list(names.values()),
        compiler_params=pltpu.CompilerParams(
            collective_id=0, has_side_effects=True, vmem_limit_bytes=60 << 20
        ),
        name="layers",
    )(node_input, graph_ids, edge_src, edge_dst, halo_send, edge_feat, w_proj, w_edge, w_qkv, w_out, w_up,
      w_down, norm_gain.transpose(1, 0, 2), norm_shift.transpose(1, 0, 2), cotangent)
    names = reduce_scratch(N, M)
    summed = pl.pallas_call(
        functools.partial(reduce_kernel, N, M, tuple(names)),
        out_shape=groups,
        in_specs=[hbm] * 3,
        out_specs=[hbm] * len(GROUPS),
        scratch_shapes=list(names.values()),
        compiler_params=pltpu.CompilerParams(
            collective_id=1, has_side_effects=True, vmem_limit_bytes=60 << 20
        ),
        name="sums",
    )(early, conv, qkv)
    outs = (act, gin, *summed, ggain, gshift)
    weights = [shape(w.shape, F32) for w in (w_proj, w_edge, w_qkv, w_out, w_up, w_down)]
    results = pl.pallas_call(
        finish_kernel,
        out_shape=[rows, rows, *weights, norm, norm],
        in_specs=[hbm] * (2 + len(GROUPS)) + [vmem] * 2,
        out_specs=[hbm] * 8 + [vmem] * 2,
        scratch_shapes=[pltpu.VMEM(s.shape, s.dtype) for s in (*groups, rows, rows, *weights)]
        + [pltpu.SemaphoreType.DMA((len(GROUPS) + 2,)), pltpu.SemaphoreType.DMA((14,))],
        compiler_params=pltpu.CompilerParams(vmem_limit_bytes=60 << 20),
        name="gradients",
    )(*outs)
    ggain, gshift = results[8].transpose(1, 0, 2), results[9].transpose(1, 0, 2)
    return (*results[:8], ggain, gshift)


BLOCK_CAP = 2048


def extended_2(block, sides, width):
    for axis, dim in sides:
        count = lax.axis_size(axis)
        forward = [(i, i + 1) for i in range(count - 1)]
        forward.append((count - 1, 0))
        backward = [(target, source) for source, target in forward]
        low = lax.ppermute(
            lax.slice_in_dim(block, block.shape[dim] - width, None, axis=dim), axis, forward
        )
        high = lax.ppermute(lax.slice_in_dim(block, 0, width, axis=dim), axis, backward)
        block = jnp.concatenate([low, block, high], axis=dim)
    return block


def block_length(total_rows, upper_limit):
    for length in range(min(total_rows, upper_limit), 0, -1):
        if total_rows % length == 0:
            return length
    return 1


def outer_product(left, right):
    return lax.dot_general(
        left, right, (((0,), (0,)), ((), ())), preferred_element_type=jnp.float32
    )


def times_transposed(left, weight):
    return lax.dot_general(
        left, weight, (((1,), (1,)), ((), ())), preferred_element_type=jnp.float32
    )


def forward_product(left, weight):
    return jnp.dot(left, weight, preferred_element_type=jnp.float32)


def silu_slope_plain(inputs):
    logistic = jax.nn.sigmoid(inputs)
    return logistic * (1.0 + inputs * (1.0 - logistic))


def normalize(inputs, gain_row, shift_row, node_total):
    batch_mean = lax.psum(jnp.sum(inputs, 0), ("nodes", "rep")) / node_total
    centred = inputs - batch_mean
    batch_var = lax.psum(jnp.sum(centred * centred, 0), ("nodes", "rep")) / node_total
    inv_std = lax.rsqrt(batch_var + NORM_EPS)
    standard = (inputs - batch_mean) * inv_std
    return (standard * gain_row + shift_row, standard, inv_std)


def normalize_back(grad_out, standard, inv_std, gain_row, node_total):
    shift_grad, gain_grad = lax.psum(
        (jnp.sum(grad_out, 0), jnp.sum(grad_out * standard, 0)), ("nodes", "rep")
    )
    grad_in = (
        gain_row
        * inv_std
        * (grad_out - shift_grad / node_total - standard * gain_grad / node_total)
    )
    return (grad_in, gain_grad, shift_grad)


def exchange_sources(outgoing):
    halo_rows = outgoing.shape[0] // 2
    grown = extended_2(outgoing, (("nodes", 0),), halo_rows)
    return jnp.concatenate([grown[:halo_rows], grown[3 * halo_rows :]], 0)


def return_sources(incoming_grad):
    halo_rows = incoming_grad.shape[0] // 2
    grown = extended_2(incoming_grad.astype(jnp.bfloat16), (("nodes", 0),), halo_rows).astype(
        incoming_grad.dtype
    )
    return jnp.concatenate([grown[:halo_rows], grown[3 * halo_rows :]], 0)


def attend_forward(query_rows, key_rows, value_rows, local_graphs, group_graphs):
    row_count = query_rows.shape[0]
    score_scale = HEAD_DIM ** (-0.5)
    queries = query_rows.reshape(row_count, HEADS, HEAD_DIM)

    def add_piece(carried, kv_piece, first_row):
        key_piece, value_piece = kv_piece
        piece_rows = key_piece.shape[0]
        block_len = block_length(piece_rows, BLOCK_CAP)

        def add_block(block_state, block_index):
            row_max, row_sum, accumulated = block_state
            block_start = block_index * block_len
            key_block = lax.dynamic_slice_in_dim(key_piece, block_start, block_len, 0).reshape(
                block_len, HEADS, HEAD_DIM
            )
            value_block = lax.dynamic_slice_in_dim(value_piece, block_start, block_len, 0).reshape(
                block_len, HEADS, HEAD_DIM
            )
            key_graphs = lax.dynamic_slice_in_dim(
                group_graphs, first_row + block_start, block_len, 0
            )
            same_graph = (local_graphs[:, None] == key_graphs[None, :])[None]
            scores = (
                jnp.einsum("qhd,khd->hqk", queries, key_block, preferred_element_type=jnp.float32)
                * score_scale
            )
            scores = jnp.where(same_graph, scores, NEG)
            new_max = jnp.maximum(row_max, jnp.max(scores, 2))
            weights = jnp.where(same_graph, jnp.exp(scores - new_max[:, :, None]), 0.0)
            factor = jnp.exp(row_max - new_max)
            row_sum = row_sum * factor + jnp.sum(weights, 2)
            contrib = jnp.einsum(
                "hqk,khd->qhd",
                weights.astype(jnp.bfloat16),
                value_block,
                preferred_element_type=jnp.float32,
            )
            accumulated = accumulated * jnp.transpose(factor)[:, :, None] + contrib
            return ((new_max, row_sum, accumulated), None)

        carried, _ = lax.scan(add_block, carried, jnp.arange(piece_rows // block_len))
        return carried

    start_state = (
        jnp.full((HEADS, row_count), NEG, jnp.float32),
        jnp.zeros((HEADS, row_count), jnp.float32),
        jnp.zeros((row_count, HEADS, HEAD_DIM), jnp.float32),
    )
    row_max, row_sum, accumulated = add_piece(
        start_state,
        (
            lax.all_gather(key_rows, "nodes", axis=0, tiled=True),
            lax.all_gather(value_rows, "nodes", axis=0, tiled=True),
        ),
        jnp.int32(0),
    )
    attn_raw = accumulated / jnp.transpose(row_sum)[:, :, None]
    log_sum = row_max + jnp.log(row_sum)
    return (attn_raw, log_sum)


def attend_backward(
    query_rows, key_rows, value_rows, grad_low, attn_raw, log_sum, local_graphs, group_graphs
):
    row_count = query_rows.shape[0]
    model_width = HEADS * HEAD_DIM
    score_scale = HEAD_DIM ** (-0.5)
    queries = query_rows.reshape(row_count, HEADS, HEAD_DIM)
    grad_heads = grad_low.reshape(row_count, HEADS, HEAD_DIM)
    row_delta = jnp.einsum("qhd,qhd->hq", grad_heads.astype(jnp.float32), attn_raw)

    def score_block(key_block, value_block, key_graphs):
        same_graph = (local_graphs[:, None] == key_graphs[None, :])[None]
        scores = (
            jnp.einsum("qhd,khd->hqk", queries, key_block, preferred_element_type=jnp.float32)
            * score_scale
        )
        attn_weights = jnp.exp(jnp.where(same_graph, scores - log_sum[:, :, None], NEG))
        grad_weights = jnp.einsum(
            "qhd,khd->hqk", grad_heads, value_block, preferred_element_type=jnp.float32
        )
        grad_scores = (attn_weights * (grad_weights - row_delta[:, :, None])).astype(jnp.bfloat16)
        return (attn_weights, grad_scores)

    def key_terms(attn_weights, grad_scores, block_len):
        grad_keys = (
            jnp.einsum("hqk,qhd->khd", grad_scores, queries, preferred_element_type=jnp.float32)
            * score_scale
        )
        grad_values = jnp.einsum(
            "hqk,qhd->khd",
            attn_weights.astype(jnp.bfloat16),
            grad_heads,
            preferred_element_type=jnp.float32,
        )
        return jnp.concatenate(
            [
                grad_keys.reshape(block_len, model_width),
                grad_values.reshape(block_len, model_width),
            ],
            1,
        )

    def query_term(grad_scores, key_block):
        return (
            jnp.einsum("hqk,khd->qhd", grad_scores, key_block, preferred_element_type=jnp.float32)
            * score_scale
        )

    group_rows = group_graphs.shape[0]

    def add_piece(carried, kv_piece, first_row):
        key_piece, value_piece = kv_piece
        piece_rows = key_piece.shape[0]
        block_len = block_length(piece_rows, BLOCK_CAP)

        def add_block(block_state, block_index):
            grad_query, buffer = block_state
            block_start = block_index * block_len
            key_block = lax.dynamic_slice_in_dim(key_piece, block_start, block_len, 0).reshape(
                block_len, HEADS, HEAD_DIM
            )
            value_block = lax.dynamic_slice_in_dim(value_piece, block_start, block_len, 0).reshape(
                block_len, HEADS, HEAD_DIM
            )
            place = first_row + block_start
            key_graphs = lax.dynamic_slice_in_dim(group_graphs, place, block_len, 0)
            attn_weights, grad_scores = score_block(key_block, value_block, key_graphs)
            grad_query = grad_query + query_term(grad_scores, key_block)
            block_terms = key_terms(attn_weights, grad_scores, block_len)
            current = lax.dynamic_slice_in_dim(buffer, place, block_len, 0)
            buffer = lax.dynamic_update_slice_in_dim(buffer, current + block_terms, place, 0)
            return ((grad_query, buffer), None)

        carried, _ = lax.scan(add_block, carried, jnp.arange(piece_rows // block_len))
        return carried

    start_state = (
        jnp.zeros((row_count, HEADS, HEAD_DIM), jnp.float32),
        jnp.zeros((group_rows, 2 * model_width), jnp.float32),
    )
    grad_query, buffer = add_piece(
        start_state,
        (
            lax.all_gather(key_rows, "nodes", axis=0, tiled=True),
            lax.all_gather(value_rows, "nodes", axis=0, tiled=True),
        ),
        jnp.int32(0),
    )
    grad_kv = lax.psum_scatter(buffer, "nodes", scatter_dimension=0, tiled=True)
    return (
        grad_query.reshape(row_count, model_width),
        grad_kv[:, :model_width],
        grad_kv[:, model_width:],
    )


def layer_forward(
    hidden, params, edge_feat, edge_src, edge_dst, halo_send, local_graphs, group_graphs, node_total
):
    w_proj, w_edge, w_qkv, w_out, w_up, w_down, norm_gains, norm_shifts = params
    row_count, model_width = hidden.shape
    hidden_low = hidden.astype(jnp.bfloat16)
    projected = forward_product(hidden_low, w_proj)
    self_term = projected[:, :model_width]
    dest_term = projected[:, 2 * model_width : 3 * model_width]
    source_rows = jnp.concatenate(
        [projected[:, model_width : 2 * model_width], projected[:, 3 * model_width :]], 1
    ).astype(jnp.bfloat16)
    incoming = exchange_sources(source_rows[halo_send])
    extended = jnp.concatenate([source_rows, incoming], 0)
    edge_rows = extended[edge_src].astype(jnp.float32)
    source_b = edge_rows[:, :model_width]
    source_e = edge_rows[:, model_width:]
    edge_proj = forward_product(edge_feat, w_edge)
    gating = jax.nn.sigmoid(dest_term[edge_dst] + source_e + edge_proj)
    numerator = jax.ops.segment_sum(gating * source_b, edge_dst, row_count)
    denominator = jax.ops.segment_sum(gating, edge_dst, row_count)
    message = self_term + numerator / (denominator + GATE_EPS)
    normed_one, standard_one, inv_one = normalize(
        message, norm_gains[0], norm_shifts[0], node_total
    )
    local_out = hidden + jax.nn.silu(normed_one)
    qkv_low = forward_product(hidden_low, w_qkv).astype(jnp.bfloat16)
    query_rows = qkv_low[:, :model_width]
    key_rows = qkv_low[:, model_width : 2 * model_width]
    value_rows = qkv_low[:, 2 * model_width :]
    attn_raw, log_sum = attend_forward(query_rows, key_rows, value_rows, local_graphs, group_graphs)
    attn_low = attn_raw.reshape(row_count, model_width).astype(jnp.bfloat16)
    attn_proj = forward_product(attn_low, w_out)
    normed_two, standard_two, inv_two = normalize(
        hidden + attn_proj, norm_gains[1], norm_shifts[1], node_total
    )
    mixed = local_out + normed_two
    mixed_low = mixed.astype(jnp.bfloat16)
    up_proj = forward_product(mixed_low, w_up)
    activated = jax.nn.silu(up_proj).astype(jnp.bfloat16)
    down_proj = forward_product(activated, w_down)
    normed_three, standard_three, inv_three = normalize(
        mixed + down_proj, norm_gains[2], norm_shifts[2], node_total
    )
    saved = (
        hidden_low,
        source_b,
        gating,
        numerator,
        denominator,
        normed_one,
        standard_one,
        inv_one,
        query_rows,
        key_rows,
        value_rows,
        attn_raw,
        log_sum,
        attn_low,
        standard_two,
        inv_two,
        mixed_low,
        up_proj,
        activated,
        standard_three,
        inv_three,
    )
    return (normed_three, saved)


def layer_backward(
    grad_out,
    params,
    saved,
    edge_feat,
    edge_src,
    edge_dst,
    halo_send,
    local_graphs,
    group_graphs,
    node_total,
):
    w_proj, w_edge, w_qkv, w_out, w_up, w_down, norm_gains, norm_shifts = params
    (
        hidden_low,
        source_b,
        gating,
        numerator,
        denominator,
        normed_one,
        standard_one,
        inv_one,
        query_rows,
        key_rows,
        value_rows,
        attn_raw,
        log_sum,
        attn_low,
        standard_two,
        inv_two,
        mixed_low,
        up_proj,
        activated,
        standard_three,
        inv_three,
    ) = saved
    row_count, model_width = grad_out.shape
    grad_three, gain_three, shift_three = normalize_back(
        grad_out, standard_three, inv_three, norm_gains[2], node_total
    )
    down_grad = grad_three.astype(jnp.bfloat16)
    grad_w_down = outer_product(activated, down_grad)
    up_grad = (times_transposed(down_grad, w_down) * silu_slope_plain(up_proj)).astype(jnp.bfloat16)
    grad_w_up = outer_product(mixed_low, up_grad)
    grad_mixed = grad_three + times_transposed(up_grad, w_up)
    grad_two, gain_two, shift_two = normalize_back(
        grad_mixed, standard_two, inv_two, norm_gains[1], node_total
    )
    out_grad = grad_two.astype(jnp.bfloat16)
    grad_w_out = outer_product(attn_low, out_grad)
    attn_grad = times_transposed(out_grad, w_out).astype(jnp.bfloat16)
    grad_query, grad_key, grad_value = attend_backward(
        query_rows, key_rows, value_rows, attn_grad, attn_raw, log_sum, local_graphs, group_graphs
    )
    qkv_grad = jnp.concatenate([grad_query, grad_key, grad_value], 1).astype(jnp.bfloat16)
    grad_w_qkv = outer_product(hidden_low, qkv_grad)
    grad_message, gain_one, shift_one = normalize_back(
        grad_mixed * silu_slope_plain(normed_one), standard_one, inv_one, norm_gains[0], node_total
    )
    shifted = denominator + GATE_EPS
    grad_numer = grad_message / shifted
    grad_denom = -grad_message * numerator / (shifted * shifted)
    numer_edge = grad_numer[edge_dst]
    grad_gate = numer_edge * source_b + grad_denom[edge_dst]
    grad_pre_edge = grad_gate * gating * (1.0 - gating)
    edge_grad = grad_pre_edge.astype(jnp.bfloat16)
    grad_w_edge = outer_product(edge_feat, edge_grad)
    grad_dest = jax.ops.segment_sum(grad_pre_edge, edge_dst, row_count)
    grad_extended = jax.ops.segment_sum(
        jnp.concatenate([numer_edge * gating, grad_pre_edge], 1),
        edge_src,
        row_count + halo_send.shape[0],
    )
    returned = return_sources(grad_extended[row_count:])
    grad_source = grad_extended[:row_count].at[halo_send].add(returned)
    proj_grad = jnp.concatenate(
        [grad_message, grad_source[:, :model_width], grad_dest, grad_source[:, model_width:]], 1
    ).astype(jnp.bfloat16)
    grad_w_proj = outer_product(hidden_low, proj_grad)
    grad_hidden = (
        grad_mixed
        + grad_two
        + times_transposed(proj_grad, w_proj)
        + times_transposed(qkv_grad, w_qkv)
    )
    weight_grads = (grad_w_proj, grad_w_edge, grad_w_qkv, grad_w_out, grad_w_up, grad_w_down)
    return (
        grad_hidden,
        weight_grads,
        jnp.stack([gain_one, gain_two, gain_three]),
        jnp.stack([shift_one, shift_two, shift_three]),
    )


def per_device(
    node_input,
    edge_feat,
    graph_ids,
    edge_src,
    edge_dst,
    halo_send,
    w_proj,
    w_edge,
    w_qkv,
    w_out,
    w_up,
    w_down,
    norm_gain,
    norm_shift,
    cotangent,
):
    group_graphs = lax.all_gather(graph_ids, "nodes", axis=0, tiled=True)
    node_total = node_input.shape[0] * lax.axis_size("nodes") * lax.axis_size("rep")
    layer_count = w_proj.shape[0]
    layer_params = [
        (
            w_proj[layer_index],
            w_edge[layer_index],
            w_qkv[layer_index],
            w_out[layer_index],
            w_up[layer_index],
            w_down[layer_index],
            norm_gain[layer_index],
            norm_shift[layer_index],
        )
        for layer_index in range(layer_count)
    ]
    hidden = node_input.astype(jnp.float32)
    saved_all = []
    for layer_index in range(layer_count):
        hidden, saved = layer_forward(
            hidden,
            layer_params[layer_index],
            edge_feat,
            edge_src,
            edge_dst,
            halo_send,
            graph_ids,
            group_graphs,
            node_total,
        )
        saved_all.append(saved)
    grad_hidden = cotangent.astype(jnp.float32)
    weight_parts = [None] * layer_count
    gain_parts = [None] * layer_count
    shift_parts = [None] * layer_count
    for layer_index in range(layer_count - 1, -1, -1):
        (
            grad_hidden,
            weight_parts[layer_index],
            gain_parts[layer_index],
            shift_parts[layer_index],
        ) = layer_backward(
            grad_hidden,
            layer_params[layer_index],
            saved_all[layer_index],
            edge_feat,
            edge_src,
            edge_dst,
            halo_send,
            graph_ids,
            group_graphs,
            node_total,
        )
    proj_local = jnp.stack([weight_parts[layer_index][0] for layer_index in range(layer_count)])
    edge_local = jnp.stack([weight_parts[layer_index][1] for layer_index in range(layer_count)])
    qkv_local = jnp.stack([weight_parts[layer_index][2] for layer_index in range(layer_count)])
    out_local = jnp.stack([weight_parts[layer_index][3] for layer_index in range(layer_count)])
    up_local = jnp.stack([weight_parts[layer_index][4] for layer_index in range(layer_count)])
    down_local = jnp.stack([weight_parts[layer_index][5] for layer_index in range(layer_count)])
    grad_proj, grad_edge, grad_qkv, grad_out, grad_up, grad_down = lax.psum(
        (proj_local, edge_local, qkv_local, out_local, up_local, down_local), ("nodes", "rep")
    )
    return (
        hidden,
        grad_hidden,
        grad_proj,
        grad_edge,
        grad_qkv,
        grad_out,
        grad_up,
        grad_down,
        jnp.stack(gain_parts),
        jnp.stack(shift_parts),
    )


def solution(mesh):
    in_specs = (
        P(("rep", "nodes"), None),
        P(("rep", "nodes"), None),
        P(("rep", "nodes")),
        P(("rep", "nodes")),
        P(("rep", "nodes")),
        P(("rep", "nodes")),
        P(),
        P(),
        P(),
        P(),
        P(),
        P(),
        P(),
        P(),
        P(("rep", "nodes"), None),
    )
    out_specs = (
        P(("rep", "nodes"), None),
        P(("rep", "nodes"), None),
        P(),
        P(),
        P(),
        P(),
        P(),
        P(),
        P(),
        P(),
    )
    N, M = mesh.shape["nodes"], mesh.shape["rep"]
    fused = N in (4, 8) and M % 2 == 0 and 512 % (16 * N * M) == 0
    return jax.shard_map(
        functools.partial(fused_device, N, M) if fused else per_device,
        mesh=mesh, in_specs=in_specs, out_specs=out_specs, check_vma=False,
    )
```

```python
import functools
import math

import jax
import jax.numpy as jnp
from jax import lax
from jax.experimental import pallas as pl
from jax.experimental.pallas import tpu as pltpu
from jax.sharding import PartitionSpec as P

HEADS = 8
HEAD_DIM = 32
NEG = -1e30
NORM_EPS = 1e-05
GATE_EPS = 1e-06
F32, BF16, I32 = jnp.float32, jnp.bfloat16, jnp.int32
MESH = pl.DeviceIdType.MESH
SYNCS = 7
GROUPS = (
    ("early", 1, 0, 2560, ("core", "y", "nodes")),
    ("conv", 1, 0, 2560, ("core", "y", "nodes")),
    ("qkv", 1, 0, 1536, ("core", "y", "nodes")),
    ("early", 0, 0, 2560, ("core", "y", "nodes")),
    ("conv", 0, 0, 2560, ("core", "y", "nodes")),
    ("qkv", 0, 0, 1024, ("rep", "nodes")),
    ("qkv", 0, 1024, 512, ("nodes", "rep")),
)


def dot(left, right):
    return lax.dot_general(
        left, right, (((1,), (0,)), ((), ())), preferred_element_type=F32
    )


def dot_nt(left, right):
    return lax.dot_general(
        left, right, (((1,), (1,)), ((), ())), preferred_element_type=F32
    )


def dot_tn(left, right):
    return lax.dot_general(
        left, right, (((0,), (0,)), ((), ())), preferred_element_type=F32
    )


def split(value):
    high = value.astype(BF16)
    return high, (value - high.astype(F32)).astype(BF16)


def select_rows(onehot, value):
    high, low = split(value)
    return dot(onehot, high) + dot(onehot, low)


def sigmoid(value):
    return 1.0 / (1.0 + jnp.exp(-value))


def silu_slope(value):
    logistic = sigmoid(value)
    return logistic * (1.0 + value * (1.0 - logistic))


def col_sum(value):
    return jnp.sum(value, axis=0, keepdims=True)


def pack(first, second, third, fourth):
    halves = []
    for row in (first, second, third, fourth):
        halves += [row[:, :128], row[:, 128:]]
    return jnp.concatenate(halves, 0)


def unpack(tile):
    return [
        jnp.concatenate([tile[2 * i : 2 * i + 1], tile[2 * i + 1 : 2 * i + 2]], 1)
        for i in range(4)
    ]


def combine_pair(tiles, count):
    mean = jnp.mean(tiles[:, 0:4], 0)
    off = tiles[:, 0:4] - mean
    return jnp.concatenate([mean, jnp.sum(tiles[:, 4:8] + count * off * off, 0)], 0)


def combine_last(tiles, count):
    mean = jnp.mean(tiles[:, 0:2], 0)
    off = tiles[:, 0:2] - mean
    return jnp.concatenate(
        [
            mean,
            jnp.sum(tiles[:, 2:4], 0),
            jnp.sum(tiles[:, 4:6] + count * off * off, 0),
            jnp.sum(tiles[:, 6:8] + off * tiles[:, 2:4], 0),
        ],
        0,
    )


def combine_sum(tiles, count):
    return jnp.sum(tiles, 0)


class Refs:
    pass


def axis_sizes(N, M):
    return dict(core=2, y=M // 2, x=2, z=N // 2, rep=M, nodes=N)


def scratch_list(N, M, L, R, E):
    NZ, NB, G = N // 2, N // 4, N * R
    D, FF, W, HH = 256, 512, 4 * R, HEADS // 2 * R
    dma = lambda *shape: pltpu.SemaphoreType.DMA(shape)
    vm = lambda dtype, *shape: pltpu.VMEM(shape, dtype)
    names = dict(
        gb=vm(BF16, L, N, R, D),
        xs=vm(BF16, L, N, R, D),
        meta=vm(I32, N, 8, 256),
        ef=vm(BF16, E, D),
        cot=vm(BF16, R, D),
        wp=vm(BF16, L, D, 4 * D),
        we=vm(BF16, L, D, D),
        wqkv=vm(BF16, L, D, 3 * D),
        wo=vm(BF16, L, D, D),
        wu=vm(BF16, L, D, FF),
        wd=vm(BF16, L, FF, D),
        st1=vm(F32, SYNCS, M * N, 8, 128),
        gain=vm(F32, L, 8, D),
        shift=vm(F32, L, 8, D),
        ggain=vm(F32, L, 8, D),
        gshift=vm(F32, L, 8, D),
        iv=vm(F32, L, 8, D),
        moff=vm(F32, N, 8, D),
        move=vm(F32, 8, D),
        T=vm(BF16, E, R),
        TT=vm(BF16, R, E),
        S=vm(BF16, E, 256),
        ST=vm(BF16, 256, E),
        efT=vm(BF16, D, E),
        HP=vm(BF16, 32, R),
        HN=vm(BF16, 32, R),
        A=vm(BF16, R, 64),
        bias=vm(F32, R, G),
        ce=vm(F32, L, E, D),
        xf=vm(F32, L + 1, R, D),
        xe=vm(BF16, L, 256, D),
        xeT=vm(BF16, D, 256),
        gate=vm(F32, L, E, D),
        bs=vm(BF16, L, E, D),
        num=vm(F32, L, R, D),
        den=vm(F32, L, R, D),
        z0=vm(F32, L, R, D),
        z1=vm(F32, L, R, D),
        z2=vm(F32, L, R, D),
        kk=vm(BF16, L, G, D),
        vv=vm(BF16, L, G, D),
        kT=vm(BF16, D, G),
        vT=vm(BF16, D, G),
        od=vm(F32, NB, R, D),
        md=vm(F32, NB, R, D),
        ld=vm(F32, NB, R, D),
        rb=vm(F32, L, NB, R, D),
        pst=vm(BF16, L, HEADS * R, G),
        oraw=vm(F32, L, R, D),
        ob=vm(BF16, L, R, D),
        mb=vm(BF16, L, R, D),
        u=vm(F32, L, R, FF),
        g=vm(BF16, L, R, FF),
        dy=vm(F32, R, D),
        dmix=vm(F32, R, D),
        dxo=vm(F32, R, D),
        dob=vm(F32, R, D),
        dq=vm(F32, R, D),
        qm=vm(BF16, L, 2, HH, 128),
        qmT=vm(BF16, 2, 128, HH),
        dom=vm(BF16, HH, 128),
        dss=vm(BF16, HH, W),
        dkv=vm(BF16, 2 * D, W),
        gkv=vm(F32, 2 * D, D),
        dce=vm(BF16, E, D),
        dproj=vm(BF16, 4, 256, D),
        dxs=vm(BF16, L, NZ, 2, R, D),
        rs1=vm(BF16, L, NZ, R, D),
        cs=vm(BF16, L, NZ, R, D),
        rs2=vm(BF16, L, NZ, R, D),
        hs=vm(BF16, L, 2, 32, D),
        hr=vm(BF16, L, 2, 32, D),
    )
    names.update(
        gs_early=vm(BF16, L, 2560, 128),
        gs_conv=vm(BF16, L, 2560, 128),
        gs_qkv=vm(BF16, L, 1536, 128),
    )
    sizes = axis_sizes(N, M)
    for g, (_, _, _, rows, stages) in enumerate(GROUPS):
        names[f"go{g}"] = vm(BF16, rows, 128)
        left = rows
        for k, axis in enumerate(stages):
            left //= sizes[axis]
            names[f"ga{g}_{k}"] = vm(BF16, sizes[axis] - 1, left, 128)
            if k < len(stages) - 1:
                names[f"gh{g}_{k}"] = vm(BF16, left, 128)
    names.update(
        ar_s=dma(len(GROUPS), 8),
        ar_r=dma(len(GROUPS), 8),
        ar_l=dma(len(GROUPS)),
        load=dma(10),
        store=dma(2),
        meta_s=dma(1),
        meta_r=dma(1),
        st1_s=dma(SYNCS),
        st1_r=dma(SYNCS),
        agc_s=dma(L, NZ),
        agc_r=dma(L, NZ),
        agp_s=dma(L, NZ),
        agp_r=dma(L, NZ),
        rsp_s=dma(L, NZ),
        rsp_r=dma(L, NZ),
        rsc_s=dma(L, NZ),
        rsc_r=dma(L, NZ),
        hal_s=dma(L, 2),
        hal_r=dma(L, 2),
    )
    return names


IN_NAMES = (
    "x_in", "ids", "edge_src", "edge_dst", "halo", "ef_h", "wp_h", "we_h", "wqkv_h", "wo_h", "wu_h", "wd_h",
    "gain_in", "shift_in", "cot_h",
)
OUT_NAMES = ("out_act", "grad_in", *(f"gout{g}" for g in range(len(GROUPS))), "ggain_out", "gshift_out")


def kernel(N, M, L, names, *args):
    r_ = Refs()
    for name, ref in zip(IN_NAMES + OUT_NAMES + tuple(names), args, strict=True):
        setattr(r_, name, ref)
    R, D = r_.x_in.shape
    E = r_.ef.shape[0]
    NZ, NB, G, W = N // 2, N // 4, N * R, 4 * R
    HK = HEADS // 2
    total = float(N * M * R)
    scale = HEAD_DIM ** -0.5
    me = lax.axis_index("nodes")
    rep = lax.axis_index("rep")
    z = me // 2
    par = me % 2
    partner = 2 * z + (1 - par)
    prev = (me + N - 1) % N
    nxt = (me + 1) % N
    zh, zl = z // 2, z % 2
    z_to = lambda t: 2 * ((zh + t // 2) % NB) + (zl + t % 2) % 2
    z_from = lambda t: 2 * ((zh + NB - t // 2) % NB) + (zl + t % 2) % 2

    def remote(src, dst, s_sem, r_sem, **where):
        return pltpu.make_async_remote_copy(
            src_ref=src, dst_ref=dst, send_sem=s_sem, recv_sem=r_sem,
            device_id=where, device_id_type=MESH,
        )

    def send(src, dst, s_sem, r_sem, **where):
        remote(src, dst, s_sem, r_sem, **where).start()

    def arrive(dst, r_sem):
        remote(dst, dst, r_sem, r_sem, nodes=partner).wait_recv()

    def sent(src, s_sem):
        remote(src, src, s_sem, s_sem, nodes=partner).wait_send()

    def when(condition, *acts):
        @pl.when(condition)
        def _():
            for act in acts:
                act()

    loads = [
        pltpu.make_async_copy(getattr(r_, f"{name}_h"), getattr(r_, name), r_.load.at[i])
        for i, name in enumerate(("ef", "we", "wqkv", "wp", "wo", "wu", "wd", "cot"))
    ]
    own_rows = pltpu.make_async_copy(r_.x_in, r_.gb.at[0, me], r_.load.at[8])
    own_rows.start()
    for load in loads:
        load.start()

    barrier = pltpu.get_barrier_semaphore()
    for dr in range(M):
        for d in range(N):
            if dr + d > 0:
                pl.semaphore_signal(barrier, inc=1, device_id={"rep": (rep + dr) % M, "nodes": (me + d) % N},
                                    device_id_type=MESH)
    pl.semaphore_wait(barrier, M * N - 1)

    def gather_start(l):
        mine = r_.gb.at[l, me]
        send(mine, mine, r_.agp_s.at[l, 0], r_.agp_r.at[l, 0], nodes=partner)
        for t in range(1, NZ):
            send(mine, mine, r_.agc_s.at[l, t], r_.agc_r.at[l, t], nodes=2 * z_to(t) + par)

    def gather_pass(l, t):
        piece = r_.gb.at[l, 2 * z_from(t) + par]
        arrive(piece, r_.agc_r.at[l, t])
        send(piece, piece, r_.agp_s.at[l, t], r_.agp_r.at[l, t], nodes=partner)

    def gather_take(l, t):
        arrive(r_.gb.at[l, 2 * z_from(t) + 1 - par], r_.agp_r.at[l, t])

    def sync_start(k, tile):
        mine = rep * N + me
        r_.st1[k, mine] = tile
        for dr in range(M):
            for d in range(N):
                if dr + d > 0:
                    send(r_.st1.at[k, mine], r_.st1.at[k, mine], r_.st1_s.at[k], r_.st1_r.at[k],
                         rep=(rep + dr) % M, nodes=(me + d) % N)

    def sync_finish(k, combine):
        arrive(r_.st1.at[k, 0 : M * N - 1], r_.st1_r.at[k])
        return unpack(combine(r_.st1[k], float(R)))

    sizes = axis_sizes(N, M)
    core, row = rep % 2, rep // 2
    places = dict(
        core=(core, lambda t: dict(rep=2 * row + t)),
        y=(row, lambda t: dict(rep=2 * t + core)),
        x=(par, lambda t: dict(nodes=2 * z + t)),
        z=(z, lambda t: dict(nodes=2 * t + par)),
        rep=(rep, lambda t: dict(rep=t)),
        nodes=(me, lambda t: dict(nodes=t)),
    )

    def reduce_step(g, step):
        name, layer, first, rows, stages = GROUPS[g]
        K = len(stages)
        gs, out = getattr(r_, f"gs_{name}").at[layer, first : first + rows], getattr(r_, f"go{g}")
        count, offset = [rows], [0]
        for axis in stages:
            count.append(count[-1] // sizes[axis])
            offset.append(offset[-1] + places[axis][0] * count[-1])
        take = lambda start, size: pl.ds(pl.multiple_of(start, 16), size)
        if 1 <= step <= K:
            k = step - 1
            got = getattr(r_, f"ga{g}_{k}")
            arrive(got, r_.ar_r.at[g, k])
            held = gs if k == 0 else getattr(r_, f"gh{g}_{k - 1}")
            index = places[stages[k]][0]
            acc = held[take(index * count[k + 1], count[k + 1])].astype(F32)
            for slot in range(sizes[stages[k]] - 1):
                acc = acc + got[slot].astype(F32)
            if step < K:
                getattr(r_, f"gh{g}_{k}")[...] = acc.astype(BF16)
            else:
                out[take(offset[K], count[K])] = acc.astype(BF16)
        elif step > K:
            k = 2 * K - step
            arrive(out.at[0 : (sizes[stages[k]] - 1) * count[k + 1]], r_.ar_r.at[g, step - 1])
        if step < K:
            held = gs if step == 0 else getattr(r_, f"gh{g}_{step - 1}")
            index, device = places[stages[step]]
            size = sizes[stages[step]]
            for d in range(1, size):
                to = (index + d) % size
                send(held.at[take(to * count[step + 1], count[step + 1])], getattr(r_, f"ga{g}_{step}").at[d - 1],
                     r_.ar_s.at[g, step], r_.ar_r.at[g, step], **device(to))
        elif step < 2 * K:
            k = 2 * K - 1 - step
            index, device = places[stages[k]]
            size = sizes[stages[k]]
            here = out.at[take(offset[k + 1], count[k + 1])]
            for d in range(1, size):
                send(here, here, r_.ar_s.at[g, step], r_.ar_r.at[g, step], **device((index + d) % size))
        else:
            pltpu.make_async_copy(out, getattr(r_, f"gout{g}"), r_.ar_l.at[g]).start()

    def reduce_drain(g):
        _, _, _, rows, stages = GROUPS[g]
        K, left = len(stages), rows
        out = getattr(r_, f"go{g}")
        for k, axis in enumerate(stages):
            left //= sizes[axis]
            for step in (k, 2 * K - 1 - k):
                sent(out.at[0 : (sizes[axis] - 1) * left], r_.ar_s.at[g, step])
        pltpu.make_async_copy(out, getattr(r_, f"gout{g}"), r_.ar_l.at[g]).wait()

    def put(buf, l, at, value):
        rows = value.shape[0]
        for c in range(value.shape[1] // 128):
            buf[l, at : at + rows] = value[:, 128 * c : 128 * (c + 1)].astype(BF16)
            at += rows
        return at

    lane_head = lax.broadcasted_iota(I32, (R, 128), 1) // HEAD_DIM

    def by_head(parts):
        out = parts[0]
        for k in range(1, HK):
            out = jnp.where(lane_head == k, parts[k], out)
        return out

    r_.meta[me] = jnp.full((8, 256), -1, I32)
    r_.meta[me, 0:1, 0:R] = r_.ids[...].reshape(1, R)
    r_.meta[me, 1:2, 0:48] = r_.halo[...].reshape(1, 48)
    for d in range(1, N):
        send(r_.meta.at[me], r_.meta.at[me], r_.meta_s.at[0], r_.meta_r.at[0], nodes=(me + d) % N)
    own_rows.wait()
    gather_start(0)

    src_row = r_.edge_src[...].reshape(1, E)
    src_row = jnp.where(src_row < R + 24, src_row, src_row + 8)
    dst_row = r_.edge_dst[...].reshape(1, E)
    src_col = jnp.broadcast_to(src_row, (128, E)).T[:, 0:1]
    dst_col = jnp.broadcast_to(dst_row, (128, E)).T[:, 0:1]
    as_mask = lambda cond: cond.astype(F32).astype(BF16)
    r_.T[...] = as_mask(dst_col == lax.broadcasted_iota(I32, (E, R), 1))
    r_.TT[...] = as_mask(dst_row == lax.broadcasted_iota(I32, (R, E), 0))
    r_.S[...] = as_mask(src_col == lax.broadcasted_iota(I32, (E, 256), 1))
    r_.ST[...] = as_mask(src_row == lax.broadcasted_iota(I32, (256, E), 0))
    loads[0].wait()
    r_.efT[...] = r_.ef[...].T
    loads[1].wait()
    for l in range(L):
        r_.ce[l] = dot(r_.ef[...], r_.we[l])
        for k in range(3):
            r_.gain[l, k : k + 1] = r_.gain_in[k, l : l + 1]
            r_.shift[l, k : k + 1] = r_.shift_in[k, l : l + 1]
    r_.xf[0] = r_.gb[0, me].astype(F32)
    r_.moff[...] = jnp.zeros((N, 8, D), F32)
    r_.move[0:1] = jnp.ones((1, D), F32)
    r_.move[1:2] = jnp.zeros((1, D), F32)
    for load in loads[2:]:
        load.wait()

    arrive(r_.meta.at[0 : N - 1], r_.meta_r.at[0])
    id_col = jnp.broadcast_to(r_.meta[me][0:1, 0:R], (128, R)).T[:, 0:1]
    id_row = jnp.concatenate([r_.meta[j][0:1, 0:R] for j in range(N)], 1)
    r_.bias[...] = jnp.where(id_col == id_row, 0.0, NEG)

    def halo_onehot(device, start):
        col = jnp.broadcast_to(r_.meta[device][1:2, 0:128], (128, 128)).T[start : start + 24, 0:1]
        hot = (col == lax.broadcasted_iota(I32, (24, R), 1)).astype(F32)
        return jnp.concatenate([hot, jnp.zeros((8, R), F32)], 0).astype(BF16)

    r_.HP[...] = halo_onehot(prev, 24)
    r_.HN[...] = halo_onehot(nxt, 0)
    r_.A[...] = as_mask(r_.meta[me][1:2, 0:64] == lax.broadcasted_iota(I32, (R, 64), 0))

    factor_exp = scale * math.log2(math.e)

    def prepare_queries(l):
        q = dot(r_.xs[l, me], r_.wqkv[l, :, :D]).astype(BF16).astype(F32)
        for hf in range(2):
            for k in range(HK):
                part = jnp.where(lane_head == k, q[:, 128 * hf : 128 * (hf + 1)], 0.0)
                r_.qm[l, hf, k * R : (k + 1) * R] = part.astype(BF16)

    def head_rows(hf, k, count=1):
        return pl.ds(pl.multiple_of((hf * HK + k) * R, 64), count * R)

    def lane_half(hf):
        return pl.ds(pl.multiple_of(hf * 128, 128), 128)

    def attention_block(l, i, middle):
        half = (zh + NB - i) % NB
        rows = pl.ds(pl.multiple_of(half * W, 128), W)
        x = r_.xs[l, pl.ds(4 * half, 4)].reshape(W, D)
        key = dot(x, r_.wqkv[l, :, D : 2 * D]).astype(BF16)
        r_.kk[l, rows] = key
        r_.kT[:, rows] = key.T
        r_.vv[l, rows] = dot(x, r_.wqkv[l, :, 2 * D :]).astype(BF16)

        def heads(hf, carry):
            lanes = lane_half(hf)
            tops, sums, outs = [], [], []
            for c in range(HK // 2):
                scores = dot(r_.qm[l, hf, 2 * c * R : 2 * (c + 1) * R], r_.kT[lanes, rows])
                for k in range(2):
                    s = scores[k * R : (k + 1) * R] + r_.bias[:, rows]
                    top = jnp.max(s, 1, keepdims=True)
                    e = jnp.exp2((s - top) * factor_exp)
                    tops.append(top)
                    sums.append(jnp.sum(e, 1, keepdims=True))
                    r_.pst[l, head_rows(hf, 2 * c + k), rows] = e.astype(BF16)
                o = dot(r_.pst[l, head_rows(hf, 2 * c, 2), rows], r_.vv[l, rows, lanes])
                outs += [o[0:R], o[R : 2 * R]]
            r_.md[i, :, lanes] = by_head([jnp.broadcast_to(v, (R, 128)) for v in tops])
            r_.ld[i, :, lanes] = by_head([jnp.broadcast_to(v, (R, 128)) for v in sums])
            r_.od[i, :, lanes] = by_head(outs)
            middle(i, hf)
            return carry

        lax.fori_loop(0, 2, heads, 0)

    def attention_end(l):
        top = r_.md[0]
        for i in range(1, NB):
            top = jnp.maximum(top, r_.md[i])
        factors = [jnp.exp2((r_.md[i] - top) * factor_exp) for i in range(NB)]
        inv = 1.0 / sum(factors[i] * r_.ld[i] for i in range(NB))
        o = jnp.zeros((R, D), F32)
        for i in range(NB):
            r_.rb[l, i] = factors[i] * inv
            o = o + factors[i] * inv * r_.od[i]
        r_.oraw[l] = o
        ob = o.astype(BF16)
        r_.ob[l] = ob
        t1 = r_.xf[l] + dot(ob, r_.wo[l])
        r_.z1[l] = t1
        mean1 = col_sum(t1) / R
        return mean1, col_sum((t1 - mean1) * (t1 - mean1))

    def convolution(l):
        xs = r_.xs
        xb = xs[l, me]
        r_.xe[l, 0:R] = xb
        r_.xe[l, R : R + 32] = dot(r_.HP[...], xs[l, prev]).astype(BF16)
        r_.xe[l, R + 32 : R + 64] = dot(r_.HN[...], xs[l, nxt]).astype(BF16)
        xe = r_.xe[l]
        tab_b = dot(xe, r_.wp[l, :, D : 2 * D]).astype(BF16)
        tab_e = dot(xe, r_.wp[l, :, 3 * D :]).astype(BF16)
        pa = dot(xb, r_.wp[l, :, 0:D])
        pd = dot(xb, r_.wp[l, :, 2 * D : 3 * D])
        bs = dot(r_.S[...], tab_b)
        r_.bs[l] = bs.astype(BF16)
        gate = sigmoid(select_rows(r_.T[...], pd) + dot(r_.S[...], tab_e) + r_.ce[l])
        r_.gate[l] = gate
        num = select_rows(r_.TT[...], gate * bs)
        den = select_rows(r_.TT[...], gate)
        r_.num[l] = num
        r_.den[l] = den
        msg = pa + num / (den + GATE_EPS)
        r_.z0[l] = msg

    def forward(l, carry):
        def ready(js):
            for j in js:
                moved = (r_.gb[l, j].astype(F32) + r_.moff[j, 0:1]) * r_.move[0:1] + r_.move[1:2]
                r_.xs[l, j] = moved.astype(BF16)

        r_.xs[l, me] = r_.xf[l].astype(BF16)
        gather_pass(l, 1)
        prepare_queries(l)
        gather_take(l, 0)
        gather_take(l, 1)
        ready([partner, 2 * z_from(1) + par, 2 * z_from(1) + 1 - par])

        def middle(i, hf):
            for t in range(2, NZ):
                when((i == 0) & (hf == t - 2), lambda: gather_pass(l, t))

        def block(i, carry):
            attention_block(l, i, middle)

            @pl.when(i == 0)
            def _():
                for t in range(2, NZ):
                    gather_take(l, t)
                ready([2 * z_from(t) + p for t in range(2, NZ) for p in range(2)])
                convolution(l)

            return carry

        lax.fori_loop(0, NB, block, 0)
        mean1, sq1 = attention_end(l)
        msg = r_.z0[l]
        mean0 = col_sum(msg) / R
        sq0 = col_sum((msg - mean0) * (msg - mean0))
        sync_start(2 * l, pack(mean0, mean1, sq0, sq1))
        mean0, mean1, sq0, sq1 = sync_finish(2 * l, combine_pair)
        inv0 = lax.rsqrt(sq0 / total + NORM_EPS)
        inv1 = lax.rsqrt(sq1 / total + NORM_EPS)
        r_.iv[l, 0:1] = inv0
        r_.iv[l, 1:2] = inv1
        z0 = (r_.z0[l] - mean0) * inv0
        z1 = (r_.z1[l] - mean1) * inv1
        r_.z0[l] = z0
        r_.z1[l] = z1
        n0 = z0 * r_.gain[l, 0:1] + r_.shift[l, 0:1]
        mix = r_.xf[l] + n0 * sigmoid(n0) + z1 * r_.gain[l, 1:2] + r_.shift[l, 1:2]
        mb = mix.astype(BF16)
        r_.mb[l] = mb
        u = dot(mb, r_.wu[l])
        r_.u[l] = u
        g = (u * sigmoid(u)).astype(BF16)
        r_.g[l] = g
        y = mix + dot(g, r_.wd[l])
        r_.z2[l] = y
        mean = col_sum(y) / R
        cent = y - mean
        k = 2 * l + 1
        dy = r_.cot[...].astype(F32)
        sync_start(k, pack(mean, col_sum(dy), col_sum(cent * cent), col_sum(dy * cent)))

        @pl.when(l < L - 1)
        def _():
            r_.gb[l + 1, me] = cent.astype(BF16)
            gather_start(l + 1)

        tot_mean, dy_sum, tot_sq, dy_cent = sync_finish(k, combine_last)
        inv2 = lax.rsqrt(tot_sq / total + NORM_EPS)
        r_.iv[l, 2:3] = inv2
        z2 = (r_.z2[l] - tot_mean) * inv2
        r_.z2[l] = z2
        gain, shift = r_.gain[l, 2:3], r_.shift[l, 2:3]
        r_.xf[l + 1] = z2 * gain + shift
        r_.gshift[l, 2:3] = dy_sum
        r_.ggain[l, 2:3] = dy_cent * inv2
        for j in range(N):
            tile = r_.st1[k, rep * N + j]
            r_.moff[j, 0:1] = jnp.concatenate([tile[0:1], tile[1:2]], 1) - tot_mean
        r_.move[0:1] = inv2 * gain
        r_.move[1:2] = shift
        return carry

    lax.fori_loop(0, L, forward, 0)
    act_copy = pltpu.make_async_copy(r_.xf.at[L], r_.out_act, r_.store.at[0])
    act_copy.start()

    def back_feed_forward(l, k):
        s2, g2 = r_.gshift[l, 2:3], r_.ggain[l, 2:3]
        d3 = r_.gain[l, 2:3] * r_.iv[l, 2:3] * (r_.dy[...] - s2 / total - r_.z2[l] * (g2 / total))
        db = d3.astype(BF16)
        dub = (dot_nt(db, r_.wd[l]) * silu_slope(r_.u[l])).astype(BF16)
        dmix = d3 + dot_nt(dub, r_.wu[l])
        r_.dmix[...] = dmix
        n0 = r_.z0[l] * r_.gain[l, 0:1] + r_.shift[l, 0:1]
        gy0 = dmix * silu_slope(n0)
        sync_start(k, pack(col_sum(dmix), col_sum(dmix * r_.z1[l]), col_sum(gy0), col_sum(gy0 * r_.z0[l])))
        at = put(r_.gs_early, l, 512, dot_tn(r_.mb[l], dub))
        put(r_.gs_early, l, at, dot_tn(r_.g[l], db))
        r_.vT[...] = r_.vv[l].T
        r_.xeT[...] = r_.xe[l].T
        for hf in range(2):
            r_.qmT[hf] = r_.qm[l, hf].T

    def back_norms(l, k):
        s1, g1, s0, g0 = sync_finish(k, combine_sum)
        r_.gshift[l, 1:2] = s1
        r_.ggain[l, 1:2] = g1
        r_.gshift[l, 0:1] = s0
        r_.ggain[l, 0:1] = g0
        dmix = r_.dmix[...]
        d2 = r_.gain[l, 1:2] * r_.iv[l, 1:2] * (dmix - s1 / total - r_.z1[l] * (g1 / total))
        dab = d2.astype(BF16)
        r_.dxo[...] = dmix + d2
        r_.dob[...] = dot_nt(dab, r_.wo[l]).astype(BF16).astype(F32)
        put(r_.gs_early, l, 0, dot_tn(r_.ob[l], dab))
        r_.gkv[...] = jnp.zeros((2 * D, D), F32)
        r_.dq[...] = jnp.zeros((R, D), F32)

    def back_attention_block(l, i, between):
        t1 = (i + 1) % NB
        half = (zh + t1) % NB
        rows = pl.ds(pl.multiple_of(half * W, 128), W)

        def heads(hf, carry):
            lanes = lane_half(hf)
            dos = r_.dob[:, lanes] * r_.rb[l, (NB - t1) % NB, :, lanes]
            prod = dos * r_.oraw[l, :, lanes]
            for k in range(HK):
                r_.dom[k * R : (k + 1) * R] = jnp.where(lane_head == k, dos, 0.0).astype(BF16)
            parts = []
            for c in range(HK // 2):
                both = slice(2 * c * R, 2 * (c + 1) * R)
                dp = dot(r_.dom[both], r_.vT[lanes, rows])
                for k in range(2):
                    h = 2 * c + k
                    delta = jnp.sum(jnp.where(lane_head == h, prod, 0.0), 1, keepdims=True)
                    ds = r_.pst[l, head_rows(hf, h), rows].astype(F32) * (dp[k * R : (k + 1) * R] - delta)
                    r_.dss[h * R : (h + 1) * R] = ds.astype(BF16)
                part = dot(r_.dss[both], r_.kk[l, rows, lanes])
                parts += [part[0:R], part[R : 2 * R]]
            r_.dq[:, lanes] += by_head(parts)
            dk = dot(r_.qmT[hf], r_.dss[...]) * scale
            r_.dkv[pl.ds(pl.multiple_of(hf * 128, 128), 128)] = dk.astype(BF16)
            dv = dot(r_.dom[...].T, r_.pst[l, head_rows(hf, 0, HK), rows])
            r_.dkv[pl.ds(pl.multiple_of(D + hf * 128, 128), 128)] = dv.astype(BF16)
            between(i, hf)
            return carry

        lax.fori_loop(0, 2, heads, 0)
        dx = dot(r_.wqkv[l, :, D:], r_.dkv[...]).T
        r_.dxs[l, pl.ds(2 * half, 2)] = dx.astype(BF16).reshape(2, 2, R, D)
        for low in range(2):
            zb = 2 * half + low
            send(r_.dxs.at[l, zb, 1 - par], r_.rs1.at[l, zb],
                 r_.rsp_s.at[l, 2 * i + low], r_.rsp_r.at[l, 2 * i + low], nodes=partner)
        r_.gkv[...] += dot(r_.dkv[...], r_.xs[l, pl.ds(4 * half, 4)].reshape(W, D))

    def pass_on(l, i, t):
        zb = z_to(t)
        arrive(r_.rs1.at[l, zb], r_.rsp_r.at[l, 2 * i + zb % 2])
        both = r_.dxs[l, zb, par].astype(F32) + r_.rs1[l, zb].astype(F32)
        r_.cs[l, zb] = both.astype(BF16)
        send(r_.cs.at[l, zb], r_.rs2.at[l, z], r_.rsc_s.at[l, t], r_.rsc_r.at[l, t], nodes=2 * zb + par)

    def back_convolution(l):
        s0, g0 = r_.gshift[l, 0:1], r_.ggain[l, 0:1]
        inv_den = 1.0 / (r_.den[l] + GATE_EPS)
        n0 = r_.z0[l] * r_.gain[l, 0:1] + r_.shift[l, 0:1]
        gy0 = r_.dmix[...] * silu_slope(n0)
        dm = r_.gain[l, 0:1] * r_.iv[l, 0:1] * (gy0 - s0 / total - r_.z0[l] * (g0 / total))
        dnum = dm * inv_den
        dden = -dnum * r_.num[l] * inv_den
        dnum_e = select_rows(r_.T[...], dnum)
        dden_e = select_rows(r_.T[...], dden)
        gate = r_.gate[l]
        dgp = (dnum_e * r_.bs[l].astype(F32) + dden_e) * gate * (1.0 - gate)
        r_.dce[...] = dgp.astype(BF16)
        dpb = select_rows(r_.ST[...], dnum_e * gate).astype(BF16)
        dpe = select_rows(r_.ST[...], dgp).astype(BF16)
        dpd = select_rows(r_.TT[...], dgp).astype(BF16)
        dmb = dm.astype(BF16)
        dxe = dot_nt(dpb, r_.wp[l, :, D : 2 * D]) + dot_nt(dpe, r_.wp[l, :, 3 * D :])
        r_.hs[l, 0] = dxe[R : R + 32].astype(BF16)
        r_.hs[l, 1] = dxe[R + 32 : R + 64].astype(BF16)
        send(r_.hs.at[l, 0], r_.hr.at[l, 1], r_.hal_s.at[l, 0], r_.hal_r.at[l, 0], nodes=prev)
        send(r_.hs.at[l, 1], r_.hr.at[l, 0], r_.hal_s.at[l, 1], r_.hal_r.at[l, 1], nodes=nxt)
        r_.dxo[...] += (
            dxe[0:R]
            + dot_nt(dmb, r_.wp[l, :, 0:D])
            + dot_nt(dpd, r_.wp[l, :, 2 * D : 3 * D])
        )
        r_.dproj[0, 0:R] = dmb
        r_.dproj[1] = dpb
        r_.dproj[2, 0:R] = dpd
        r_.dproj[3] = dpe

    def conv_weight_grads(l):
        at = 0
        for c in range(4):
            width = R if c % 2 == 0 else 256
            at = put(r_.gs_conv, l, at, dot(r_.xeT[:, 0:width], r_.dproj[c, 0:width]))
        put(r_.gs_conv, l, at, dot(r_.efT[...], r_.dce[...]))

    def back_input(l):
        dx = r_.dxo[...]
        arrive(r_.rs1.at[l, z], r_.rsp_r.at[l, 2 * (NB - 1) + zl])
        dx = dx + r_.dxs[l, z, par].astype(F32) + r_.rs1[l, z].astype(F32)
        for t in range(1, NZ):
            c = z_from(t)
            arrive(r_.rs2.at[l, c], r_.rsc_r.at[l, t])
            dx = dx + r_.rs2[l, c].astype(F32)
        arrive(r_.hr.at[l, 0], r_.hal_r.at[l, 1])
        arrive(r_.hr.at[l, 1], r_.hal_r.at[l, 0])
        back = jnp.concatenate(
            [r_.hr[l, 0].astype(F32)[0:24], r_.hr[l, 1].astype(F32)[0:24], jnp.zeros((16, D), F32)], 0
        )
        return dx + dot(r_.A[...], back.astype(BF16))

    r_.dy[...] = r_.cot[...].astype(F32)

    E1, C1, Q1, E0, C0, QK0, V0 = range(len(GROUPS))

    def steps(*pairs):
        return [functools.partial(reduce_step, g, k) for g, k in pairs]

    def backward(b, carry):
        l = L - 1 - b
        first, last = b == 0, b == L - 1
        k = 4 + 2 * b
        when(last, *steps((Q1, 1)))
        back_feed_forward(l, k)
        when(last, *steps((C1, 2), (Q1, 2), (E1, 5)))
        back_norms(l, k)
        when(first, *steps((E1, 0)))
        when(last, *steps((E0, 0), (C1, 3), (Q1, 3)))

        def between(i, hf):
            when(first & (i == 0) & (hf == 1), *steps((E1, 1)))
            when(first & (i == 1) & (hf == 1), *steps((E1, 3)))
            when(last & (i == 0) & (hf == 1), *steps((E0, 1)))
            when(last & (i == 1) & (hf == 0), *steps((C1, 5), (Q1, 5)))
            when(last & (i == 1) & (hf == 1), *steps((E0, 3), (C0, 1)))
            for t in range(2, NZ):
                when((i == 1) & (hf == 0), functools.partial(pass_on, l, 0, t))

        def block(i, carry):
            back_attention_block(l, i, between)

            @pl.when(i == 0)
            def _():
                when(last, *steps((C1, 4), (Q1, 4), (E1, 6)))
                back_convolution(l)
                when(first, *steps((E1, 2)))
                when(last, functools.partial(conv_weight_grads, l), *steps((C0, 0), (E0, 2)))

            return carry

        lax.fori_loop(0, NB, block, 0)
        dqb = (r_.dq[...] * scale).astype(BF16)
        r_.dxo[...] += dot_nt(dqb, r_.wqkv[l, :, 0:D])
        when(first, functools.partial(conv_weight_grads, l), *steps((C1, 0)))
        at = put(r_.gs_qkv, l, 0, dot(r_.xeT[:, 0:R], dqb))
        put(r_.gs_qkv, l, at, r_.gkv[...].T)
        when(last, *steps((QK0, 0), (V0, 0), (C0, 2)))
        pass_on(l, NB - 1, 1)
        when(last, *steps((C1, 6), (Q1, 6), (E0, 4)))
        dx = back_input(l)
        r_.dy[...] = dx

        @pl.when(first)
        def _():
            below = L - 2
            zero_row = jnp.zeros((1, D), F32)
            sync_start(5, pack(col_sum(dx), col_sum(dx * r_.z2[below]), zero_row, zero_row))
            for step in steps((C1, 1), (Q1, 0), (E1, 4)):
                step()
            s2, g2, _, _ = sync_finish(5, combine_sum)
            r_.gshift[below, 2:3] = s2
            r_.ggain[below, 2:3] = g2

        return carry

    lax.fori_loop(0, L, backward, 0)
    in_copy = pltpu.make_async_copy(r_.dy, r_.grad_in, r_.store.at[1])
    in_copy.start()
    for step in steps(
        (V0, 1), (QK0, 1), (C0, 3), (E0, 5),
        (V0, 2), (QK0, 2), (C0, 4), (E0, 6),
        (V0, 3), (QK0, 3), (C0, 5),
        (V0, 4), (QK0, 4), (C0, 6),
    ):
        step()
    for l in range(L):
        for k in range(3):
            r_.ggain_out[k, l : l + 1] = r_.ggain[l, k : k + 1]
            r_.gshift_out[k, l : l + 1] = r_.gshift[l, k : k + 1]
    for g in range(len(GROUPS)):
        reduce_drain(g)
    sent(r_.meta.at[0 : N - 1], r_.meta_s.at[0])
    for k in range(SYNCS):
        sent(r_.st1.at[k, 0 : M * N - 1], r_.st1_s.at[k])
    for l in range(L):
        for t in range(NZ):
            sent(r_.gb.at[l, 0], r_.agp_s.at[l, t])
            sent(r_.rs1.at[l, 0], r_.rsp_s.at[l, t])
            if t > 0:
                sent(r_.gb.at[l, 0], r_.agc_s.at[l, t])
                sent(r_.rs1.at[l, 0], r_.rsc_s.at[l, t])
        for side in range(2):
            sent(r_.hs.at[l, 0], r_.hal_s.at[l, side])
    act_copy.wait()
    in_copy.wait()


def finish_kernel(act_h, gin_h, *refs):
    n = len(GROUPS)
    held, (ggain_h, gshift_h), refs = refs[:n], refs[n : n + 2], refs[n + 2 :]
    act_o, gin_o, proj_o, edge_o, qkv_o, out_o, up_o, down_o, ggain_o, gshift_o = refs[:10]
    summed, refs = refs[10 : 10 + n], refs[10 + n :]
    act, gin, proj, edge, qkv, out, up, down, in_sem, out_sem = refs
    loads = [
        pltpu.make_async_copy(src, dst, in_sem.at[i])
        for i, (src, dst) in enumerate(zip(held + (act_h, gin_h), summed + (act, gin), strict=True))
    ]
    for load in loads:
        load.start()
    ggain_o[...] = ggain_h[...]
    gshift_o[...] = gshift_h[...]
    stores = []

    def store(src, dst):
        copy = pltpu.make_async_copy(src, dst, out_sem.at[len(stores)])
        copy.start()
        stores.append(copy)

    def widen(dst, l, g, at, first=0, last=None):
        rows = dst.shape[1]
        for c in range(first, dst.shape[2] // 128 if last is None else last):
            dst[l, :, 128 * c : 128 * (c + 1)] = summed[g][at : at + rows].astype(F32)
            at += rows
        return at

    for g, (name, l, first, rows, _) in enumerate(GROUPS):
        loads[g].wait()
        if name == "early":
            at = widen(out, l, g, 0)
            store(out.at[l], out_o.at[l])
            at = widen(up, l, g, at)
            store(up.at[l], up_o.at[l])
            widen(down, l, g, at)
            store(down.at[l], down_o.at[l])
        elif name == "conv":
            at = widen(proj, l, g, 0)
            store(proj.at[l], proj_o.at[l])
            widen(edge, l, g, at)
            store(edge.at[l], edge_o.at[l])
        else:
            widen(qkv, l, g, 0, first // 256, (first + rows) // 256)
            if first + rows == 1536:
                store(qkv.at[l], qkv_o.at[l])
    for i, (src, dst) in enumerate(((act, act_o), (gin, gin_o))):
        loads[n + i].wait()
        store(src, dst)
    for copy in stores:
        copy.wait()


def fused_device(
    N, M, node_input, edge_feat, graph_ids, edge_src, edge_dst, halo_send, w_proj, w_edge, w_qkv,
    w_out, w_up, w_down, norm_gain, norm_shift, cotangent,
):
    R, D = node_input.shape
    E = edge_feat.shape[0]
    L = w_proj.shape[0]
    names = scratch_list(N, M, L, R, E)
    vmem = pl.BlockSpec(memory_space=pltpu.VMEM)
    hbm = pl.BlockSpec(memory_space=pltpu.HBM)
    shape = jax.ShapeDtypeStruct
    rows = shape((R, D), F32)
    norm = shape((3, L, D), F32)
    groups = [shape((rows_g, 128), BF16) for _, _, _, rows_g, _ in GROUPS]
    outs = pl.pallas_call(
        functools.partial(kernel, N, M, L, tuple(names)),
        out_shape=[rows, rows, *groups, norm, norm],
        in_specs=[hbm] + [vmem] * 4 + [hbm] * 7 + [vmem] * 2 + [hbm],
        out_specs=[hbm] * (2 + len(GROUPS)) + [vmem] * 2,
        scratch_shapes=list(names.values()),
        compiler_params=pltpu.CompilerParams(
            collective_id=0, has_side_effects=True, vmem_limit_bytes=60 << 20
        ),
        name="layers",
    )(node_input, graph_ids, edge_src, edge_dst, halo_send, edge_feat, w_proj, w_edge, w_qkv, w_out, w_up,
      w_down, norm_gain.transpose(1, 0, 2), norm_shift.transpose(1, 0, 2), cotangent)
    weights = [shape(w.shape, F32) for w in (w_proj, w_edge, w_qkv, w_out, w_up, w_down)]
    results = pl.pallas_call(
        finish_kernel,
        out_shape=[rows, rows, *weights, norm, norm],
        in_specs=[hbm] * (2 + len(GROUPS)) + [vmem] * 2,
        out_specs=[hbm] * 8 + [vmem] * 2,
        scratch_shapes=[pltpu.VMEM(s.shape, s.dtype) for s in (*groups, rows, rows, *weights)]
        + [pltpu.SemaphoreType.DMA((len(GROUPS) + 2,)), pltpu.SemaphoreType.DMA((14,))],
        compiler_params=pltpu.CompilerParams(vmem_limit_bytes=60 << 20),
        name="gradients",
    )(*outs)
    ggain, gshift = results[8].transpose(1, 0, 2), results[9].transpose(1, 0, 2)
    return (*results[:8], ggain, gshift)


BLOCK_CAP = 2048


def extended_2(block, sides, width):
    for axis, dim in sides:
        count = lax.axis_size(axis)
        forward = [(i, i + 1) for i in range(count - 1)]
        forward.append((count - 1, 0))
        backward = [(target, source) for source, target in forward]
        low = lax.ppermute(
            lax.slice_in_dim(block, block.shape[dim] - width, None, axis=dim), axis, forward
        )
        high = lax.ppermute(lax.slice_in_dim(block, 0, width, axis=dim), axis, backward)
        block = jnp.concatenate([low, block, high], axis=dim)
    return block


def block_length(total_rows, upper_limit):
    for length in range(min(total_rows, upper_limit), 0, -1):
        if total_rows % length == 0:
            return length
    return 1


def outer_product(left, right):
    return lax.dot_general(
        left, right, (((0,), (0,)), ((), ())), preferred_element_type=jnp.float32
    )


def times_transposed(left, weight):
    return lax.dot_general(
        left, weight, (((1,), (1,)), ((), ())), preferred_element_type=jnp.float32
    )


def forward_product(left, weight):
    return jnp.dot(left, weight, preferred_element_type=jnp.float32)


def silu_slope_plain(inputs):
    logistic = jax.nn.sigmoid(inputs)
    return logistic * (1.0 + inputs * (1.0 - logistic))


def normalize(inputs, gain_row, shift_row, node_total):
    batch_mean = lax.psum(jnp.sum(inputs, 0), ("nodes", "rep")) / node_total
    centred = inputs - batch_mean
    batch_var = lax.psum(jnp.sum(centred * centred, 0), ("nodes", "rep")) / node_total
    inv_std = lax.rsqrt(batch_var + NORM_EPS)
    standard = (inputs - batch_mean) * inv_std
    return (standard * gain_row + shift_row, standard, inv_std)


def normalize_back(grad_out, standard, inv_std, gain_row, node_total):
    shift_grad, gain_grad = lax.psum(
        (jnp.sum(grad_out, 0), jnp.sum(grad_out * standard, 0)), ("nodes", "rep")
    )
    grad_in = (
        gain_row
        * inv_std
        * (grad_out - shift_grad / node_total - standard * gain_grad / node_total)
    )
    return (grad_in, gain_grad, shift_grad)


def exchange_sources(outgoing):
    halo_rows = outgoing.shape[0] // 2
    grown = extended_2(outgoing, (("nodes", 0),), halo_rows)
    return jnp.concatenate([grown[:halo_rows], grown[3 * halo_rows :]], 0)


def return_sources(incoming_grad):
    halo_rows = incoming_grad.shape[0] // 2
    grown = extended_2(incoming_grad.astype(jnp.bfloat16), (("nodes", 0),), halo_rows).astype(
        incoming_grad.dtype
    )
    return jnp.concatenate([grown[:halo_rows], grown[3 * halo_rows :]], 0)


def attend_forward(query_rows, key_rows, value_rows, local_graphs, group_graphs):
    row_count = query_rows.shape[0]
    score_scale = HEAD_DIM ** (-0.5)
    queries = query_rows.reshape(row_count, HEADS, HEAD_DIM)

    def add_piece(carried, kv_piece, first_row):
        key_piece, value_piece = kv_piece
        piece_rows = key_piece.shape[0]
        block_len = block_length(piece_rows, BLOCK_CAP)

        def add_block(block_state, block_index):
            row_max, row_sum, accumulated = block_state
            block_start = block_index * block_len
            key_block = lax.dynamic_slice_in_dim(key_piece, block_start, block_len, 0).reshape(
                block_len, HEADS, HEAD_DIM
            )
            value_block = lax.dynamic_slice_in_dim(value_piece, block_start, block_len, 0).reshape(
                block_len, HEADS, HEAD_DIM
            )
            key_graphs = lax.dynamic_slice_in_dim(
                group_graphs, first_row + block_start, block_len, 0
            )
            same_graph = (local_graphs[:, None] == key_graphs[None, :])[None]
            scores = (
                jnp.einsum("qhd,khd->hqk", queries, key_block, preferred_element_type=jnp.float32)
                * score_scale
            )
            scores = jnp.where(same_graph, scores, NEG)
            new_max = jnp.maximum(row_max, jnp.max(scores, 2))
            weights = jnp.where(same_graph, jnp.exp(scores - new_max[:, :, None]), 0.0)
            factor = jnp.exp(row_max - new_max)
            row_sum = row_sum * factor + jnp.sum(weights, 2)
            contrib = jnp.einsum(
                "hqk,khd->qhd",
                weights.astype(jnp.bfloat16),
                value_block,
                preferred_element_type=jnp.float32,
            )
            accumulated = accumulated * jnp.transpose(factor)[:, :, None] + contrib
            return ((new_max, row_sum, accumulated), None)

        carried, _ = lax.scan(add_block, carried, jnp.arange(piece_rows // block_len))
        return carried

    start_state = (
        jnp.full((HEADS, row_count), NEG, jnp.float32),
        jnp.zeros((HEADS, row_count), jnp.float32),
        jnp.zeros((row_count, HEADS, HEAD_DIM), jnp.float32),
    )
    row_max, row_sum, accumulated = add_piece(
        start_state,
        (
            lax.all_gather(key_rows, "nodes", axis=0, tiled=True),
            lax.all_gather(value_rows, "nodes", axis=0, tiled=True),
        ),
        jnp.int32(0),
    )
    attn_raw = accumulated / jnp.transpose(row_sum)[:, :, None]
    log_sum = row_max + jnp.log(row_sum)
    return (attn_raw, log_sum)


def attend_backward(
    query_rows, key_rows, value_rows, grad_low, attn_raw, log_sum, local_graphs, group_graphs
):
    row_count = query_rows.shape[0]
    model_width = HEADS * HEAD_DIM
    score_scale = HEAD_DIM ** (-0.5)
    queries = query_rows.reshape(row_count, HEADS, HEAD_DIM)
    grad_heads = grad_low.reshape(row_count, HEADS, HEAD_DIM)
    row_delta = jnp.einsum("qhd,qhd->hq", grad_heads.astype(jnp.float32), attn_raw)

    def score_block(key_block, value_block, key_graphs):
        same_graph = (local_graphs[:, None] == key_graphs[None, :])[None]
        scores = (
            jnp.einsum("qhd,khd->hqk", queries, key_block, preferred_element_type=jnp.float32)
            * score_scale
        )
        attn_weights = jnp.exp(jnp.where(same_graph, scores - log_sum[:, :, None], NEG))
        grad_weights = jnp.einsum(
            "qhd,khd->hqk", grad_heads, value_block, preferred_element_type=jnp.float32
        )
        grad_scores = (attn_weights * (grad_weights - row_delta[:, :, None])).astype(jnp.bfloat16)
        return (attn_weights, grad_scores)

    def key_terms(attn_weights, grad_scores, block_len):
        grad_keys = (
            jnp.einsum("hqk,qhd->khd", grad_scores, queries, preferred_element_type=jnp.float32)
            * score_scale
        )
        grad_values = jnp.einsum(
            "hqk,qhd->khd",
            attn_weights.astype(jnp.bfloat16),
            grad_heads,
            preferred_element_type=jnp.float32,
        )
        return jnp.concatenate(
            [
                grad_keys.reshape(block_len, model_width),
                grad_values.reshape(block_len, model_width),
            ],
            1,
        )

    def query_term(grad_scores, key_block):
        return (
            jnp.einsum("hqk,khd->qhd", grad_scores, key_block, preferred_element_type=jnp.float32)
            * score_scale
        )

    group_rows = group_graphs.shape[0]

    def add_piece(carried, kv_piece, first_row):
        key_piece, value_piece = kv_piece
        piece_rows = key_piece.shape[0]
        block_len = block_length(piece_rows, BLOCK_CAP)

        def add_block(block_state, block_index):
            grad_query, buffer = block_state
            block_start = block_index * block_len
            key_block = lax.dynamic_slice_in_dim(key_piece, block_start, block_len, 0).reshape(
                block_len, HEADS, HEAD_DIM
            )
            value_block = lax.dynamic_slice_in_dim(value_piece, block_start, block_len, 0).reshape(
                block_len, HEADS, HEAD_DIM
            )
            place = first_row + block_start
            key_graphs = lax.dynamic_slice_in_dim(group_graphs, place, block_len, 0)
            attn_weights, grad_scores = score_block(key_block, value_block, key_graphs)
            grad_query = grad_query + query_term(grad_scores, key_block)
            block_terms = key_terms(attn_weights, grad_scores, block_len)
            current = lax.dynamic_slice_in_dim(buffer, place, block_len, 0)
            buffer = lax.dynamic_update_slice_in_dim(buffer, current + block_terms, place, 0)
            return ((grad_query, buffer), None)

        carried, _ = lax.scan(add_block, carried, jnp.arange(piece_rows // block_len))
        return carried

    start_state = (
        jnp.zeros((row_count, HEADS, HEAD_DIM), jnp.float32),
        jnp.zeros((group_rows, 2 * model_width), jnp.float32),
    )
    grad_query, buffer = add_piece(
        start_state,
        (
            lax.all_gather(key_rows, "nodes", axis=0, tiled=True),
            lax.all_gather(value_rows, "nodes", axis=0, tiled=True),
        ),
        jnp.int32(0),
    )
    grad_kv = lax.psum_scatter(buffer, "nodes", scatter_dimension=0, tiled=True)
    return (
        grad_query.reshape(row_count, model_width),
        grad_kv[:, :model_width],
        grad_kv[:, model_width:],
    )


def layer_forward(
    hidden, params, edge_feat, edge_src, edge_dst, halo_send, local_graphs, group_graphs, node_total
):
    w_proj, w_edge, w_qkv, w_out, w_up, w_down, norm_gains, norm_shifts = params
    row_count, model_width = hidden.shape
    hidden_low = hidden.astype(jnp.bfloat16)
    projected = forward_product(hidden_low, w_proj)
    self_term = projected[:, :model_width]
    dest_term = projected[:, 2 * model_width : 3 * model_width]
    source_rows = jnp.concatenate(
        [projected[:, model_width : 2 * model_width], projected[:, 3 * model_width :]], 1
    ).astype(jnp.bfloat16)
    incoming = exchange_sources(source_rows[halo_send])
    extended = jnp.concatenate([source_rows, incoming], 0)
    edge_rows = extended[edge_src].astype(jnp.float32)
    source_b = edge_rows[:, :model_width]
    source_e = edge_rows[:, model_width:]
    edge_proj = forward_product(edge_feat, w_edge)
    gating = jax.nn.sigmoid(dest_term[edge_dst] + source_e + edge_proj)
    numerator = jax.ops.segment_sum(gating * source_b, edge_dst, row_count)
    denominator = jax.ops.segment_sum(gating, edge_dst, row_count)
    message = self_term + numerator / (denominator + GATE_EPS)
    normed_one, standard_one, inv_one = normalize(
        message, norm_gains[0], norm_shifts[0], node_total
    )
    local_out = hidden + jax.nn.silu(normed_one)
    qkv_low = forward_product(hidden_low, w_qkv).astype(jnp.bfloat16)
    query_rows = qkv_low[:, :model_width]
    key_rows = qkv_low[:, model_width : 2 * model_width]
    value_rows = qkv_low[:, 2 * model_width :]
    attn_raw, log_sum = attend_forward(query_rows, key_rows, value_rows, local_graphs, group_graphs)
    attn_low = attn_raw.reshape(row_count, model_width).astype(jnp.bfloat16)
    attn_proj = forward_product(attn_low, w_out)
    normed_two, standard_two, inv_two = normalize(
        hidden + attn_proj, norm_gains[1], norm_shifts[1], node_total
    )
    mixed = local_out + normed_two
    mixed_low = mixed.astype(jnp.bfloat16)
    up_proj = forward_product(mixed_low, w_up)
    activated = jax.nn.silu(up_proj).astype(jnp.bfloat16)
    down_proj = forward_product(activated, w_down)
    normed_three, standard_three, inv_three = normalize(
        mixed + down_proj, norm_gains[2], norm_shifts[2], node_total
    )
    saved = (
        hidden_low,
        source_b,
        gating,
        numerator,
        denominator,
        normed_one,
        standard_one,
        inv_one,
        query_rows,
        key_rows,
        value_rows,
        attn_raw,
        log_sum,
        attn_low,
        standard_two,
        inv_two,
        mixed_low,
        up_proj,
        activated,
        standard_three,
        inv_three,
    )
    return (normed_three, saved)


def layer_backward(
    grad_out,
    params,
    saved,
    edge_feat,
    edge_src,
    edge_dst,
    halo_send,
    local_graphs,
    group_graphs,
    node_total,
):
    w_proj, w_edge, w_qkv, w_out, w_up, w_down, norm_gains, norm_shifts = params
    (
        hidden_low,
        source_b,
        gating,
        numerator,
        denominator,
        normed_one,
        standard_one,
        inv_one,
        query_rows,
        key_rows,
        value_rows,
        attn_raw,
        log_sum,
        attn_low,
        standard_two,
        inv_two,
        mixed_low,
        up_proj,
        activated,
        standard_three,
        inv_three,
    ) = saved
    row_count, model_width = grad_out.shape
    grad_three, gain_three, shift_three = normalize_back(
        grad_out, standard_three, inv_three, norm_gains[2], node_total
    )
    down_grad = grad_three.astype(jnp.bfloat16)
    grad_w_down = outer_product(activated, down_grad)
    up_grad = (times_transposed(down_grad, w_down) * silu_slope_plain(up_proj)).astype(jnp.bfloat16)
    grad_w_up = outer_product(mixed_low, up_grad)
    grad_mixed = grad_three + times_transposed(up_grad, w_up)
    grad_two, gain_two, shift_two = normalize_back(
        grad_mixed, standard_two, inv_two, norm_gains[1], node_total
    )
    out_grad = grad_two.astype(jnp.bfloat16)
    grad_w_out = outer_product(attn_low, out_grad)
    attn_grad = times_transposed(out_grad, w_out).astype(jnp.bfloat16)
    grad_query, grad_key, grad_value = attend_backward(
        query_rows, key_rows, value_rows, attn_grad, attn_raw, log_sum, local_graphs, group_graphs
    )
    qkv_grad = jnp.concatenate([grad_query, grad_key, grad_value], 1).astype(jnp.bfloat16)
    grad_w_qkv = outer_product(hidden_low, qkv_grad)
    grad_message, gain_one, shift_one = normalize_back(
        grad_mixed * silu_slope_plain(normed_one), standard_one, inv_one, norm_gains[0], node_total
    )
    shifted = denominator + GATE_EPS
    grad_numer = grad_message / shifted
    grad_denom = -grad_message * numerator / (shifted * shifted)
    numer_edge = grad_numer[edge_dst]
    grad_gate = numer_edge * source_b + grad_denom[edge_dst]
    grad_pre_edge = grad_gate * gating * (1.0 - gating)
    edge_grad = grad_pre_edge.astype(jnp.bfloat16)
    grad_w_edge = outer_product(edge_feat, edge_grad)
    grad_dest = jax.ops.segment_sum(grad_pre_edge, edge_dst, row_count)
    grad_extended = jax.ops.segment_sum(
        jnp.concatenate([numer_edge * gating, grad_pre_edge], 1),
        edge_src,
        row_count + halo_send.shape[0],
    )
    returned = return_sources(grad_extended[row_count:])
    grad_source = grad_extended[:row_count].at[halo_send].add(returned)
    proj_grad = jnp.concatenate(
        [grad_message, grad_source[:, :model_width], grad_dest, grad_source[:, model_width:]], 1
    ).astype(jnp.bfloat16)
    grad_w_proj = outer_product(hidden_low, proj_grad)
    grad_hidden = (
        grad_mixed
        + grad_two
        + times_transposed(proj_grad, w_proj)
        + times_transposed(qkv_grad, w_qkv)
    )
    weight_grads = (grad_w_proj, grad_w_edge, grad_w_qkv, grad_w_out, grad_w_up, grad_w_down)
    return (
        grad_hidden,
        weight_grads,
        jnp.stack([gain_one, gain_two, gain_three]),
        jnp.stack([shift_one, shift_two, shift_three]),
    )


def per_device(
    node_input,
    edge_feat,
    graph_ids,
    edge_src,
    edge_dst,
    halo_send,
    w_proj,
    w_edge,
    w_qkv,
    w_out,
    w_up,
    w_down,
    norm_gain,
    norm_shift,
    cotangent,
):
    group_graphs = lax.all_gather(graph_ids, "nodes", axis=0, tiled=True)
    node_total = node_input.shape[0] * lax.axis_size("nodes") * lax.axis_size("rep")
    layer_count = w_proj.shape[0]
    layer_params = [
        (
            w_proj[layer_index],
            w_edge[layer_index],
            w_qkv[layer_index],
            w_out[layer_index],
            w_up[layer_index],
            w_down[layer_index],
            norm_gain[layer_index],
            norm_shift[layer_index],
        )
        for layer_index in range(layer_count)
    ]
    hidden = node_input.astype(jnp.float32)
    saved_all = []
    for layer_index in range(layer_count):
        hidden, saved = layer_forward(
            hidden,
            layer_params[layer_index],
            edge_feat,
            edge_src,
            edge_dst,
            halo_send,
            graph_ids,
            group_graphs,
            node_total,
        )
        saved_all.append(saved)
    grad_hidden = cotangent.astype(jnp.float32)
    weight_parts = [None] * layer_count
    gain_parts = [None] * layer_count
    shift_parts = [None] * layer_count
    for layer_index in range(layer_count - 1, -1, -1):
        (
            grad_hidden,
            weight_parts[layer_index],
            gain_parts[layer_index],
            shift_parts[layer_index],
        ) = layer_backward(
            grad_hidden,
            layer_params[layer_index],
            saved_all[layer_index],
            edge_feat,
            edge_src,
            edge_dst,
            halo_send,
            graph_ids,
            group_graphs,
            node_total,
        )
    proj_local = jnp.stack([weight_parts[layer_index][0] for layer_index in range(layer_count)])
    edge_local = jnp.stack([weight_parts[layer_index][1] for layer_index in range(layer_count)])
    qkv_local = jnp.stack([weight_parts[layer_index][2] for layer_index in range(layer_count)])
    out_local = jnp.stack([weight_parts[layer_index][3] for layer_index in range(layer_count)])
    up_local = jnp.stack([weight_parts[layer_index][4] for layer_index in range(layer_count)])
    down_local = jnp.stack([weight_parts[layer_index][5] for layer_index in range(layer_count)])
    grad_proj, grad_edge, grad_qkv, grad_out, grad_up, grad_down = lax.psum(
        (proj_local, edge_local, qkv_local, out_local, up_local, down_local), ("nodes", "rep")
    )
    return (
        hidden,
        grad_hidden,
        grad_proj,
        grad_edge,
        grad_qkv,
        grad_out,
        grad_up,
        grad_down,
        jnp.stack(gain_parts),
        jnp.stack(shift_parts),
    )


def solution(mesh):
    in_specs = (
        P(("rep", "nodes"), None),
        P(("rep", "nodes"), None),
        P(("rep", "nodes")),
        P(("rep", "nodes")),
        P(("rep", "nodes")),
        P(("rep", "nodes")),
        P(),
        P(),
        P(),
        P(),
        P(),
        P(),
        P(),
        P(),
        P(("rep", "nodes"), None),
    )
    out_specs = (
        P(("rep", "nodes"), None),
        P(("rep", "nodes"), None),
        P(),
        P(),
        P(),
        P(),
        P(),
        P(),
        P(),
        P(),
    )
    N, M = mesh.shape["nodes"], mesh.shape["rep"]
    fused = N in (4, 8) and M % 2 == 0 and 512 % (16 * N * M) == 0
    return jax.shard_map(
        functools.partial(fused_device, N, M) if fused else per_device,
        mesh=mesh, in_specs=in_specs, out_specs=out_specs, check_vma=False,
    )
```

```python
import functools
import math

import jax
import jax.numpy as jnp
from jax import lax
from jax.experimental import pallas as pl
from jax.experimental.pallas import tpu as pltpu
from jax.sharding import PartitionSpec as P

HEADS = 8
HEAD_DIM = 32
NEG = -1e30
NORM_EPS = 1e-05
GATE_EPS = 1e-06
F32, BF16, I32 = jnp.float32, jnp.bfloat16, jnp.int32
MESH = pl.DeviceIdType.MESH
SYNCS = 7
GROUPS = (
    ("early", 1, 0, 2560, ("core", "y", "nodes")),
    ("conv", 1, 0, 2560, ("core", "y", "nodes")),
    ("qkv", 1, 0, 1536, ("core", "y", "nodes")),
    ("early", 0, 0, 2560, ("core", "y", "nodes")),
    ("conv", 0, 0, 2560, ("core", "y", "nodes")),
    ("qkv", 0, 0, 1024, ("rep", "nodes")),
    ("qkv", 0, 1024, 512, ("nodes", "rep")),
)


def dot(left, right):
    return lax.dot_general(
        left, right, (((1,), (0,)), ((), ())), preferred_element_type=F32
    )


def dot_nt(left, right):
    return lax.dot_general(
        left, right, (((1,), (1,)), ((), ())), preferred_element_type=F32
    )


def dot_tn(left, right):
    return lax.dot_general(
        left, right, (((0,), (0,)), ((), ())), preferred_element_type=F32
    )


def split(value):
    high = value.astype(BF16)
    return high, (value - high.astype(F32)).astype(BF16)


def select_rows(onehot, value):
    high, low = split(value)
    return dot(onehot, high) + dot(onehot, low)


def sigmoid(value):
    return 1.0 / (1.0 + jnp.exp(-value))


def silu_slope(value):
    logistic = sigmoid(value)
    return logistic * (1.0 + value * (1.0 - logistic))


def col_sum(value):
    return jnp.sum(value, axis=0, keepdims=True)


def pack(first, second, third, fourth):
    halves = []
    for row in (first, second, third, fourth):
        halves += [row[:, :128], row[:, 128:]]
    return jnp.concatenate(halves, 0)


def unpack(tile):
    return [
        jnp.concatenate([tile[2 * i : 2 * i + 1], tile[2 * i + 1 : 2 * i + 2]], 1)
        for i in range(4)
    ]


def combine_pair(tiles, count):
    mean = jnp.mean(tiles[:, 0:4], 0)
    off = tiles[:, 0:4] - mean
    return jnp.concatenate([mean, jnp.sum(tiles[:, 4:8] + count * off * off, 0)], 0)


def combine_last(tiles, count):
    mean = jnp.mean(tiles[:, 0:2], 0)
    off = tiles[:, 0:2] - mean
    return jnp.concatenate(
        [
            mean,
            jnp.sum(tiles[:, 2:4], 0),
            jnp.sum(tiles[:, 4:6] + count * off * off, 0),
            jnp.sum(tiles[:, 6:8] + off * tiles[:, 2:4], 0),
        ],
        0,
    )


def combine_sum(tiles, count):
    return jnp.sum(tiles, 0)


class Refs:
    pass


def axis_sizes(N, M):
    return dict(core=2, y=M // 2, x=2, z=N // 2, rep=M, nodes=N)


def scratch_list(N, M, L, R, E):
    NZ, NB, G = N // 2, N // 4, N * R
    D, FF, W, HH = 256, 512, 4 * R, HEADS // 2 * R
    dma = lambda *shape: pltpu.SemaphoreType.DMA(shape)
    vm = lambda dtype, *shape: pltpu.VMEM(shape, dtype)
    names = dict(
        gb=vm(BF16, L, N, R, D),
        xs=vm(BF16, L, N, R, D),
        meta=vm(I32, N, 8, 256),
        ef=vm(BF16, E, D),
        cot=vm(BF16, R, D),
        wp=vm(BF16, L, D, 4 * D),
        we=vm(BF16, L, D, D),
        wqkv=vm(BF16, L, D, 3 * D),
        wo=vm(BF16, L, D, D),
        wu=vm(BF16, L, D, FF),
        wd=vm(BF16, L, FF, D),
        st1=vm(F32, SYNCS, M * N, 8, 128),
        gain=vm(F32, L, 8, D),
        shift=vm(F32, L, 8, D),
        ggain=vm(F32, L, 8, D),
        gshift=vm(F32, L, 8, D),
        iv=vm(F32, L, 8, D),
        moff=vm(F32, N, 8, D),
        move=vm(F32, 8, D),
        T=vm(BF16, E, R),
        TT=vm(BF16, R, E),
        S=vm(BF16, E, 256),
        ST=vm(BF16, 256, E),
        efT=vm(BF16, D, E),
        HP=vm(BF16, 32, R),
        HN=vm(BF16, 32, R),
        A=vm(BF16, R, 64),
        bias=vm(F32, R, G),
        ce=vm(F32, L, E, D),
        xf=vm(F32, L + 1, R, D),
        xe=vm(BF16, L, 256, D),
        xeT=vm(BF16, D, 256),
        gate=vm(F32, L, E, D),
        bs=vm(BF16, L, E, D),
        num=vm(F32, L, R, D),
        den=vm(F32, L, R, D),
        z0=vm(F32, L, R, D),
        z1=vm(F32, L, R, D),
        z2=vm(F32, L, R, D),
        kk=vm(BF16, L, G, D),
        vv=vm(BF16, L, G, D),
        kT=vm(BF16, D, G),
        vT=vm(BF16, D, G),
        od=vm(F32, NB, R, D),
        md=vm(F32, NB, R, D),
        ld=vm(F32, NB, R, D),
        rb=vm(F32, L, NB, R, D),
        pst=vm(BF16, L, HEADS * R, G),
        oraw=vm(F32, L, R, D),
        ob=vm(BF16, L, R, D),
        mb=vm(BF16, L, R, D),
        u=vm(F32, L, R, FF),
        g=vm(BF16, L, R, FF),
        dy=vm(F32, R, D),
        dmix=vm(F32, R, D),
        dxo=vm(F32, R, D),
        dob=vm(F32, R, D),
        dq=vm(F32, R, D),
        qm=vm(BF16, L, 2, HH, 128),
        qmT=vm(BF16, 2, 128, HH),
        dom=vm(BF16, HH, 128),
        dss=vm(BF16, HH, W),
        dkv=vm(BF16, 2 * D, W),
        gkv=vm(F32, 2 * D, D),
        dce=vm(BF16, E, D),
        dproj=vm(BF16, 4, 256, D),
        dxs=vm(BF16, L, NZ, 2, R, D),
        rs1=vm(BF16, L, NZ, R, D),
        cs=vm(BF16, L, NZ, R, D),
        rs2=vm(BF16, L, NZ, R, D),
        ro=vm(BF16, L, 3, R, D),
        hs=vm(BF16, L, 2, 32, D),
        hr=vm(BF16, L, 2, 32, D),
    )
    names.update(
        gs_early=vm(BF16, L, 2560, 128),
        gs_conv=vm(BF16, L, 2560, 128),
        gs_qkv=vm(BF16, L, 1536, 128),
    )
    sizes = axis_sizes(N, M)
    for g, (_, _, _, rows, stages) in enumerate(GROUPS):
        names[f"go{g}"] = vm(BF16, rows, 128)
        left = rows
        for k, axis in enumerate(stages):
            left //= sizes[axis]
            names[f"ga{g}_{k}"] = vm(BF16, sizes[axis] - 1, left, 128)
            if k < len(stages) - 1:
                names[f"gh{g}_{k}"] = vm(BF16, left, 128)
    names.update(
        ar_s=dma(len(GROUPS), 8),
        ar_r=dma(len(GROUPS), 8),
        ar_l=dma(len(GROUPS)),
        load=dma(10),
        store=dma(2),
        meta_s=dma(1),
        meta_r=dma(1),
        st1_s=dma(SYNCS),
        st1_r=dma(SYNCS),
        agc_s=dma(L, NZ),
        agc_r=dma(L, NZ),
        agp_s=dma(L, NZ),
        agp_r=dma(L, NZ),
        rsp_s=dma(L, NZ),
        rsp_r=dma(L, NZ),
        ro_s=dma(L, 3),
        ro_r=dma(L, 3),
        rsc_s=dma(L, NZ),
        rsc_r=dma(L, NZ),
        hal_s=dma(L, 2),
        hal_r=dma(L, 2),
    )
    return names


IN_NAMES = (
    "x_in", "ids", "edge_src", "edge_dst", "halo", "ef_h", "wp_h", "we_h", "wqkv_h", "wo_h", "wu_h", "wd_h",
    "gain_in", "shift_in", "cot_h",
)
OUT_NAMES = ("out_act", "grad_in", *(f"gout{g}" for g in range(len(GROUPS))), "ggain_out", "gshift_out")


def kernel(N, M, L, names, *args):
    r_ = Refs()
    for name, ref in zip(IN_NAMES + OUT_NAMES + tuple(names), args, strict=True):
        setattr(r_, name, ref)
    R, D = r_.x_in.shape
    E = r_.ef.shape[0]
    NZ, NB, G, W = N // 2, N // 4, N * R, 4 * R
    HK = HEADS // 2
    total = float(N * M * R)
    scale = HEAD_DIM ** -0.5
    me = lax.axis_index("nodes")
    rep = lax.axis_index("rep")
    z = me // 2
    par = me % 2
    partner = 2 * z + (1 - par)
    prev = (me + N - 1) % N
    nxt = (me + 1) % N
    zh, zl = z // 2, z % 2
    z_to = lambda t: 2 * ((zh + t // 2) % NB) + (zl + t % 2) % 2
    z_from = lambda t: 2 * ((zh + NB - t // 2) % NB) + (zl + t % 2) % 2

    def remote(src, dst, s_sem, r_sem, **where):
        return pltpu.make_async_remote_copy(
            src_ref=src, dst_ref=dst, send_sem=s_sem, recv_sem=r_sem,
            device_id=where, device_id_type=MESH,
        )

    def send(src, dst, s_sem, r_sem, **where):
        remote(src, dst, s_sem, r_sem, **where).start()

    def arrive(dst, r_sem):
        remote(dst, dst, r_sem, r_sem, nodes=partner).wait_recv()

    def sent(src, s_sem):
        remote(src, src, s_sem, s_sem, nodes=partner).wait_send()

    def when(condition, *acts):
        @pl.when(condition)
        def _():
            for act in acts:
                act()

    loads = [
        pltpu.make_async_copy(getattr(r_, f"{name}_h"), getattr(r_, name), r_.load.at[i])
        for i, name in enumerate(("ef", "we", "wqkv", "wp", "wo", "wu", "wd", "cot"))
    ]
    own_rows = pltpu.make_async_copy(r_.x_in, r_.gb.at[0, me], r_.load.at[8])
    own_rows.start()
    for load in loads:
        load.start()

    barrier = pltpu.get_barrier_semaphore()
    for dr in range(M):
        for d in range(N):
            if dr + d > 0:
                pl.semaphore_signal(barrier, inc=1, device_id={"rep": (rep + dr) % M, "nodes": (me + d) % N},
                                    device_id_type=MESH)
    pl.semaphore_wait(barrier, M * N - 1)

    def gather_start(l):
        mine = r_.gb.at[l, me]
        send(mine, mine, r_.agp_s.at[l, 0], r_.agp_r.at[l, 0], nodes=partner)
        send(mine, mine, r_.agc_s.at[l, 1], r_.agc_r.at[l, 1], nodes=2 * z_to(1) + par)
        send(mine, mine, r_.agp_s.at[l, 1], r_.agp_r.at[l, 1], nodes=2 * z_to(1) + 1 - par)
        for t in range(2, NZ):
            send(mine, mine, r_.agc_s.at[l, t], r_.agc_r.at[l, t], nodes=2 * z_to(t) + par)

    def gather_pass(l, t):
        piece = r_.gb.at[l, 2 * z_from(t) + par]
        arrive(piece, r_.agc_r.at[l, t])
        send(piece, piece, r_.agp_s.at[l, t], r_.agp_r.at[l, t], nodes=partner)

    def gather_take(l, t):
        arrive(r_.gb.at[l, 2 * z_from(t) + 1 - par], r_.agp_r.at[l, t])

    def sync_start(k, tile):
        mine = rep * N + me
        r_.st1[k, mine] = tile
        for dr in range(M):
            for d in range(N):
                if dr + d > 0:
                    send(r_.st1.at[k, mine], r_.st1.at[k, mine], r_.st1_s.at[k], r_.st1_r.at[k],
                         rep=(rep + dr) % M, nodes=(me + d) % N)

    def sync_finish(k, combine):
        arrive(r_.st1.at[k, 0 : M * N - 1], r_.st1_r.at[k])
        return unpack(combine(r_.st1[k], float(R)))

    sizes = axis_sizes(N, M)
    core, row = rep % 2, rep // 2
    places = dict(
        core=(core, lambda t: dict(rep=2 * row + t)),
        y=(row, lambda t: dict(rep=2 * t + core)),
        x=(par, lambda t: dict(nodes=2 * z + t)),
        z=(z, lambda t: dict(nodes=2 * t + par)),
        rep=(rep, lambda t: dict(rep=t)),
        nodes=(me, lambda t: dict(nodes=t)),
    )

    def reduce_step(g, step):
        name, layer, first, rows, stages = GROUPS[g]
        K = len(stages)
        gs, out = getattr(r_, f"gs_{name}").at[layer, first : first + rows], getattr(r_, f"go{g}")
        count, offset = [rows], [0]
        for axis in stages:
            count.append(count[-1] // sizes[axis])
            offset.append(offset[-1] + places[axis][0] * count[-1])
        take = lambda start, size: pl.ds(pl.multiple_of(start, 16), size)
        if 1 <= step <= K:
            k = step - 1
            got = getattr(r_, f"ga{g}_{k}")
            arrive(got, r_.ar_r.at[g, k])
            held = gs if k == 0 else getattr(r_, f"gh{g}_{k - 1}")
            index = places[stages[k]][0]
            acc = held[take(index * count[k + 1], count[k + 1])].astype(F32)
            for slot in range(sizes[stages[k]] - 1):
                acc = acc + got[slot].astype(F32)
            if step < K:
                getattr(r_, f"gh{g}_{k}")[...] = acc.astype(BF16)
            else:
                out[take(offset[K], count[K])] = acc.astype(BF16)
        elif step > K:
            k = 2 * K - step
            arrive(out.at[0 : (sizes[stages[k]] - 1) * count[k + 1]], r_.ar_r.at[g, step - 1])
        if step < K:
            held = gs if step == 0 else getattr(r_, f"gh{g}_{step - 1}")
            index, device = places[stages[step]]
            size = sizes[stages[step]]
            for d in range(1, size):
                to = (index + d) % size
                send(held.at[take(to * count[step + 1], count[step + 1])], getattr(r_, f"ga{g}_{step}").at[d - 1],
                     r_.ar_s.at[g, step], r_.ar_r.at[g, step], **device(to))
        elif step < 2 * K:
            k = 2 * K - 1 - step
            index, device = places[stages[k]]
            size = sizes[stages[k]]
            here = out.at[take(offset[k + 1], count[k + 1])]
            for d in range(1, size):
                send(here, here, r_.ar_s.at[g, step], r_.ar_r.at[g, step], **device((index + d) % size))
        else:
            pltpu.make_async_copy(out, getattr(r_, f"gout{g}"), r_.ar_l.at[g]).start()

    def reduce_drain(g):
        _, _, _, rows, stages = GROUPS[g]
        K, left = len(stages), rows
        out = getattr(r_, f"go{g}")
        for k, axis in enumerate(stages):
            left //= sizes[axis]
            for step in (k, 2 * K - 1 - k):
                sent(out.at[0 : (sizes[axis] - 1) * left], r_.ar_s.at[g, step])
        pltpu.make_async_copy(out, getattr(r_, f"gout{g}"), r_.ar_l.at[g]).wait()

    def put(buf, l, at, value):
        rows = value.shape[0]
        for c in range(value.shape[1] // 128):
            buf[l, at : at + rows] = value[:, 128 * c : 128 * (c + 1)].astype(BF16)
            at += rows
        return at

    lane_head = lax.broadcasted_iota(I32, (R, 128), 1) // HEAD_DIM

    def by_head(parts):
        out = parts[0]
        for k in range(1, HK):
            out = jnp.where(lane_head == k, parts[k], out)
        return out

    r_.meta[me] = jnp.full((8, 256), -1, I32)
    r_.meta[me, 0:1, 0:R] = r_.ids[...].reshape(1, R)
    r_.meta[me, 1:2, 0:48] = r_.halo[...].reshape(1, 48)
    for d in range(1, N):
        send(r_.meta.at[me], r_.meta.at[me], r_.meta_s.at[0], r_.meta_r.at[0], nodes=(me + d) % N)
    own_rows.wait()
    gather_start(0)

    src_row = r_.edge_src[...].reshape(1, E)
    src_row = jnp.where(src_row < R + 24, src_row, src_row + 8)
    dst_row = r_.edge_dst[...].reshape(1, E)
    src_col = jnp.broadcast_to(src_row, (128, E)).T[:, 0:1]
    dst_col = jnp.broadcast_to(dst_row, (128, E)).T[:, 0:1]
    as_mask = lambda cond: cond.astype(F32).astype(BF16)
    r_.T[...] = as_mask(dst_col == lax.broadcasted_iota(I32, (E, R), 1))
    r_.TT[...] = as_mask(dst_row == lax.broadcasted_iota(I32, (R, E), 0))
    r_.S[...] = as_mask(src_col == lax.broadcasted_iota(I32, (E, 256), 1))
    r_.ST[...] = as_mask(src_row == lax.broadcasted_iota(I32, (256, E), 0))
    loads[0].wait()
    r_.efT[...] = r_.ef[...].T
    loads[1].wait()
    for l in range(L):
        r_.ce[l] = dot(r_.ef[...], r_.we[l])
        for k in range(3):
            r_.gain[l, k : k + 1] = r_.gain_in[k, l : l + 1]
            r_.shift[l, k : k + 1] = r_.shift_in[k, l : l + 1]
    r_.xf[0] = r_.gb[0, me].astype(F32)
    r_.moff[...] = jnp.zeros((N, 8, D), F32)
    r_.move[0:1] = jnp.ones((1, D), F32)
    r_.move[1:2] = jnp.zeros((1, D), F32)
    for load in loads[2:]:
        load.wait()

    arrive(r_.meta.at[0 : N - 1], r_.meta_r.at[0])
    id_col = jnp.broadcast_to(r_.meta[me][0:1, 0:R], (128, R)).T[:, 0:1]
    id_row = jnp.concatenate([r_.meta[j][0:1, 0:R] for j in range(N)], 1)
    r_.bias[...] = jnp.where(id_col == id_row, 0.0, NEG)

    def halo_onehot(device, start):
        col = jnp.broadcast_to(r_.meta[device][1:2, 0:128], (128, 128)).T[start : start + 24, 0:1]
        hot = (col == lax.broadcasted_iota(I32, (24, R), 1)).astype(F32)
        return jnp.concatenate([hot, jnp.zeros((8, R), F32)], 0).astype(BF16)

    r_.HP[...] = halo_onehot(prev, 24)
    r_.HN[...] = halo_onehot(nxt, 0)
    r_.A[...] = as_mask(r_.meta[me][1:2, 0:64] == lax.broadcasted_iota(I32, (R, 64), 0))

    factor_exp = scale * math.log2(math.e)

    def prepare_queries(l):
        q = dot(r_.xs[l, me], r_.wqkv[l, :, :D]).astype(BF16).astype(F32)
        for hf in range(2):
            for k in range(HK):
                part = jnp.where(lane_head == k, q[:, 128 * hf : 128 * (hf + 1)], 0.0)
                r_.qm[l, hf, k * R : (k + 1) * R] = part.astype(BF16)

    def head_rows(hf, k, count=1):
        return pl.ds(pl.multiple_of((hf * HK + k) * R, 64), count * R)

    def lane_half(hf):
        return pl.ds(pl.multiple_of(hf * 128, 128), 128)

    def attention_block(l, i, middle):
        half = (zh + NB - i) % NB
        rows = pl.ds(pl.multiple_of(half * W, 128), W)
        x = r_.xs[l, pl.ds(4 * half, 4)].reshape(W, D)
        key = dot(x, r_.wqkv[l, :, D : 2 * D]).astype(BF16)
        r_.kk[l, rows] = key
        r_.kT[:, rows] = key.T
        r_.vv[l, rows] = dot(x, r_.wqkv[l, :, 2 * D :]).astype(BF16)

        def heads(hf, carry):
            lanes = lane_half(hf)
            tops, sums, outs = [], [], []
            for c in range(HK // 2):
                scores = dot(r_.qm[l, hf, 2 * c * R : 2 * (c + 1) * R], r_.kT[lanes, rows])
                for k in range(2):
                    s = scores[k * R : (k + 1) * R] + r_.bias[:, rows]
                    top = jnp.max(s, 1, keepdims=True)
                    e = jnp.exp2((s - top) * factor_exp)
                    tops.append(top)
                    sums.append(jnp.sum(e, 1, keepdims=True))
                    r_.pst[l, head_rows(hf, 2 * c + k), rows] = e.astype(BF16)
                o = dot(r_.pst[l, head_rows(hf, 2 * c, 2), rows], r_.vv[l, rows, lanes])
                outs += [o[0:R], o[R : 2 * R]]
            r_.md[i, :, lanes] = by_head([jnp.broadcast_to(v, (R, 128)) for v in tops])
            r_.ld[i, :, lanes] = by_head([jnp.broadcast_to(v, (R, 128)) for v in sums])
            r_.od[i, :, lanes] = by_head(outs)
            middle(i, hf)
            return carry

        lax.fori_loop(0, 2, heads, 0)

    def attention_end(l):
        top = r_.md[0]
        for i in range(1, NB):
            top = jnp.maximum(top, r_.md[i])
        factors = [jnp.exp2((r_.md[i] - top) * factor_exp) for i in range(NB)]
        inv = 1.0 / sum(factors[i] * r_.ld[i] for i in range(NB))
        o = jnp.zeros((R, D), F32)
        for i in range(NB):
            r_.rb[l, i] = factors[i] * inv
            o = o + factors[i] * inv * r_.od[i]
        r_.oraw[l] = o
        ob = o.astype(BF16)
        r_.ob[l] = ob
        t1 = r_.xf[l] + dot(ob, r_.wo[l])
        r_.z1[l] = t1
        mean1 = col_sum(t1) / R
        return mean1, col_sum((t1 - mean1) * (t1 - mean1))

    def convolution(l):
        xs = r_.xs
        xb = xs[l, me]
        r_.xe[l, 0:R] = xb
        r_.xe[l, R : R + 32] = dot(r_.HP[...], xs[l, prev]).astype(BF16)
        r_.xe[l, R + 32 : R + 64] = dot(r_.HN[...], xs[l, nxt]).astype(BF16)
        xe = r_.xe[l]
        tab_b = dot(xe, r_.wp[l, :, D : 2 * D]).astype(BF16)
        tab_e = dot(xe, r_.wp[l, :, 3 * D :]).astype(BF16)
        pa = dot(xb, r_.wp[l, :, 0:D])
        pd = dot(xb, r_.wp[l, :, 2 * D : 3 * D])
        bs = dot(r_.S[...], tab_b)
        r_.bs[l] = bs.astype(BF16)
        gate = sigmoid(select_rows(r_.T[...], pd) + dot(r_.S[...], tab_e) + r_.ce[l])
        r_.gate[l] = gate
        num = select_rows(r_.TT[...], gate * bs)
        den = select_rows(r_.TT[...], gate)
        r_.num[l] = num
        r_.den[l] = den
        msg = pa + num / (den + GATE_EPS)
        r_.z0[l] = msg

    def forward(l, carry):
        def ready(js):
            for j in js:
                moved = (r_.gb[l, j].astype(F32) + r_.moff[j, 0:1]) * r_.move[0:1] + r_.move[1:2]
                r_.xs[l, j] = moved.astype(BF16)

        r_.xs[l, me] = r_.xf[l].astype(BF16)
        prepare_queries(l)
        arrive(r_.gb.at[l, 2 * z_from(1) + par], r_.agc_r.at[l, 1])
        gather_take(l, 0)
        gather_take(l, 1)
        ready([partner, 2 * z_from(1) + par, 2 * z_from(1) + 1 - par])

        def middle(i, hf):
            when((i == 0) & (hf == 0), *[functools.partial(gather_pass, l, t) for t in range(2, NZ)])

        def block(i, carry):
            attention_block(l, i, middle)

            @pl.when(i == 0)
            def _():
                for t in range(2, NZ):
                    gather_take(l, t)
                ready([2 * z_from(t) + p for t in range(2, NZ) for p in range(2)])
                convolution(l)

            return carry

        lax.fori_loop(0, NB, block, 0)
        mean1, sq1 = attention_end(l)
        msg = r_.z0[l]
        mean0 = col_sum(msg) / R
        sq0 = col_sum((msg - mean0) * (msg - mean0))
        sync_start(2 * l, pack(mean0, mean1, sq0, sq1))
        mean0, mean1, sq0, sq1 = sync_finish(2 * l, combine_pair)
        inv0 = lax.rsqrt(sq0 / total + NORM_EPS)
        inv1 = lax.rsqrt(sq1 / total + NORM_EPS)
        r_.iv[l, 0:1] = inv0
        r_.iv[l, 1:2] = inv1
        z0 = (r_.z0[l] - mean0) * inv0
        z1 = (r_.z1[l] - mean1) * inv1
        r_.z0[l] = z0
        r_.z1[l] = z1
        n0 = z0 * r_.gain[l, 0:1] + r_.shift[l, 0:1]
        mix = r_.xf[l] + n0 * sigmoid(n0) + z1 * r_.gain[l, 1:2] + r_.shift[l, 1:2]
        mb = mix.astype(BF16)
        r_.mb[l] = mb
        u = dot(mb, r_.wu[l])
        r_.u[l] = u
        g = (u * sigmoid(u)).astype(BF16)
        r_.g[l] = g
        y = mix + dot(g, r_.wd[l])
        r_.z2[l] = y
        mean = col_sum(y) / R
        cent = y - mean
        k = 2 * l + 1
        dy = r_.cot[...].astype(F32)
        sync_start(k, pack(mean, col_sum(dy), col_sum(cent * cent), col_sum(dy * cent)))

        @pl.when(l < L - 1)
        def _():
            r_.gb[l + 1, me] = cent.astype(BF16)
            gather_start(l + 1)

        tot_mean, dy_sum, tot_sq, dy_cent = sync_finish(k, combine_last)
        inv2 = lax.rsqrt(tot_sq / total + NORM_EPS)
        r_.iv[l, 2:3] = inv2
        z2 = (r_.z2[l] - tot_mean) * inv2
        r_.z2[l] = z2
        gain, shift = r_.gain[l, 2:3], r_.shift[l, 2:3]
        r_.xf[l + 1] = z2 * gain + shift
        r_.gshift[l, 2:3] = dy_sum
        r_.ggain[l, 2:3] = dy_cent * inv2
        for j in range(N):
            tile = r_.st1[k, rep * N + j]
            r_.moff[j, 0:1] = jnp.concatenate([tile[0:1], tile[1:2]], 1) - tot_mean
        r_.move[0:1] = inv2 * gain
        r_.move[1:2] = shift
        return carry

    lax.fori_loop(0, L, forward, 0)
    act_copy = pltpu.make_async_copy(r_.xf.at[L], r_.out_act, r_.store.at[0])
    act_copy.start()

    def back_feed_forward(l, k):
        s2, g2 = r_.gshift[l, 2:3], r_.ggain[l, 2:3]
        d3 = r_.gain[l, 2:3] * r_.iv[l, 2:3] * (r_.dy[...] - s2 / total - r_.z2[l] * (g2 / total))
        db = d3.astype(BF16)
        dub = (dot_nt(db, r_.wd[l]) * silu_slope(r_.u[l])).astype(BF16)
        dmix = d3 + dot_nt(dub, r_.wu[l])
        r_.dmix[...] = dmix
        n0 = r_.z0[l] * r_.gain[l, 0:1] + r_.shift[l, 0:1]
        gy0 = dmix * silu_slope(n0)
        sync_start(k, pack(col_sum(dmix), col_sum(dmix * r_.z1[l]), col_sum(gy0), col_sum(gy0 * r_.z0[l])))
        at = put(r_.gs_early, l, 512, dot_tn(r_.mb[l], dub))
        put(r_.gs_early, l, at, dot_tn(r_.g[l], db))
        r_.vT[...] = r_.vv[l].T
        r_.xeT[...] = r_.xe[l].T
        for hf in range(2):
            r_.qmT[hf] = r_.qm[l, hf].T

    def back_norms(l, k):
        s1, g1, s0, g0 = sync_finish(k, combine_sum)
        r_.gshift[l, 1:2] = s1
        r_.ggain[l, 1:2] = g1
        r_.gshift[l, 0:1] = s0
        r_.ggain[l, 0:1] = g0
        dmix = r_.dmix[...]
        d2 = r_.gain[l, 1:2] * r_.iv[l, 1:2] * (dmix - s1 / total - r_.z1[l] * (g1 / total))
        dab = d2.astype(BF16)
        r_.dxo[...] = dmix + d2
        r_.dob[...] = dot_nt(dab, r_.wo[l]).astype(BF16).astype(F32)
        put(r_.gs_early, l, 0, dot_tn(r_.ob[l], dab))
        r_.gkv[...] = jnp.zeros((2 * D, D), F32)
        r_.dq[...] = jnp.zeros((R, D), F32)

    def back_attention_block(l, i, between):
        t1 = (i + 1) % NB
        half = (zh + t1) % NB
        rows = pl.ds(pl.multiple_of(half * W, 128), W)

        def heads(hf, carry):
            lanes = lane_half(hf)
            dos = r_.dob[:, lanes] * r_.rb[l, (NB - t1) % NB, :, lanes]
            prod = dos * r_.oraw[l, :, lanes]
            for k in range(HK):
                r_.dom[k * R : (k + 1) * R] = jnp.where(lane_head == k, dos, 0.0).astype(BF16)
            parts = []
            for c in range(HK // 2):
                both = slice(2 * c * R, 2 * (c + 1) * R)
                dp = dot(r_.dom[both], r_.vT[lanes, rows])
                for k in range(2):
                    h = 2 * c + k
                    delta = jnp.sum(jnp.where(lane_head == h, prod, 0.0), 1, keepdims=True)
                    ds = r_.pst[l, head_rows(hf, h), rows].astype(F32) * (dp[k * R : (k + 1) * R] - delta)
                    r_.dss[h * R : (h + 1) * R] = ds.astype(BF16)
                part = dot(r_.dss[both], r_.kk[l, rows, lanes])
                parts += [part[0:R], part[R : 2 * R]]
            r_.dq[:, lanes] += by_head(parts)
            dk = dot(r_.qmT[hf], r_.dss[...]) * scale
            r_.dkv[pl.ds(pl.multiple_of(hf * 128, 128), 128)] = dk.astype(BF16)
            dv = dot(r_.dom[...].T, r_.pst[l, head_rows(hf, 0, HK), rows])
            r_.dkv[pl.ds(pl.multiple_of(D + hf * 128, 128), 128)] = dv.astype(BF16)
            between(i, hf)
            return carry

        lax.fori_loop(0, 2, heads, 0)
        dx = dot(r_.wqkv[l, :, D:], r_.dkv[...]).T
        r_.dxs[l, pl.ds(2 * half, 2)] = dx.astype(BF16).reshape(2, 2, R, D)

        @pl.when(i < NB - 1)
        def _():
            for low in range(2):
                zb = 2 * half + low
                send(r_.dxs.at[l, zb, 1 - par], r_.rs1.at[l, zb],
                     r_.rsp_s.at[l, 2 * i + low], r_.rsp_r.at[l, 2 * i + low], nodes=partner)

        @pl.when(i == NB - 1)
        def _():
            near = z_to(1)
            send(r_.dxs.at[l, z, 1 - par], r_.ro.at[l, 0], r_.ro_s.at[l, 0], r_.ro_r.at[l, 0], nodes=partner)
            send(r_.dxs.at[l, near, par], r_.ro.at[l, 1], r_.ro_s.at[l, 1], r_.ro_r.at[l, 1], nodes=2 * near + par)
            send(r_.dxs.at[l, near, 1 - par], r_.ro.at[l, 2], r_.ro_s.at[l, 2], r_.ro_r.at[l, 2],
                 nodes=2 * near + 1 - par)

        r_.gkv[...] += dot(r_.dkv[...], r_.xs[l, pl.ds(4 * half, 4)].reshape(W, D))

    def pass_on(l, i, t):
        zb = z_to(t)
        arrive(r_.rs1.at[l, zb], r_.rsp_r.at[l, 2 * i + zb % 2])
        both = r_.dxs[l, zb, par].astype(F32) + r_.rs1[l, zb].astype(F32)
        r_.cs[l, zb] = both.astype(BF16)
        send(r_.cs.at[l, zb], r_.rs2.at[l, z], r_.rsc_s.at[l, t], r_.rsc_r.at[l, t], nodes=2 * zb + par)

    def back_convolution(l):
        s0, g0 = r_.gshift[l, 0:1], r_.ggain[l, 0:1]
        inv_den = 1.0 / (r_.den[l] + GATE_EPS)
        n0 = r_.z0[l] * r_.gain[l, 0:1] + r_.shift[l, 0:1]
        gy0 = r_.dmix[...] * silu_slope(n0)
        dm = r_.gain[l, 0:1] * r_.iv[l, 0:1] * (gy0 - s0 / total - r_.z0[l] * (g0 / total))
        dnum = dm * inv_den
        dden = -dnum * r_.num[l] * inv_den
        dnum_e = select_rows(r_.T[...], dnum)
        dden_e = select_rows(r_.T[...], dden)
        gate = r_.gate[l]
        dgp = (dnum_e * r_.bs[l].astype(F32) + dden_e) * gate * (1.0 - gate)
        r_.dce[...] = dgp.astype(BF16)
        dpb = select_rows(r_.ST[...], dnum_e * gate).astype(BF16)
        dpe = select_rows(r_.ST[...], dgp).astype(BF16)
        dpd = select_rows(r_.TT[...], dgp).astype(BF16)
        dmb = dm.astype(BF16)
        dxe = dot_nt(dpb, r_.wp[l, :, D : 2 * D]) + dot_nt(dpe, r_.wp[l, :, 3 * D :])
        r_.hs[l, 0] = dxe[R : R + 32].astype(BF16)
        r_.hs[l, 1] = dxe[R + 32 : R + 64].astype(BF16)
        send(r_.hs.at[l, 0], r_.hr.at[l, 1], r_.hal_s.at[l, 0], r_.hal_r.at[l, 0], nodes=prev)
        send(r_.hs.at[l, 1], r_.hr.at[l, 0], r_.hal_s.at[l, 1], r_.hal_r.at[l, 1], nodes=nxt)
        r_.dxo[...] += (
            dxe[0:R]
            + dot_nt(dmb, r_.wp[l, :, 0:D])
            + dot_nt(dpd, r_.wp[l, :, 2 * D : 3 * D])
        )
        r_.dproj[0, 0:R] = dmb
        r_.dproj[1] = dpb
        r_.dproj[2, 0:R] = dpd
        r_.dproj[3] = dpe

    def conv_weight_grads(l):
        at = 0
        for c in range(4):
            width = R if c % 2 == 0 else 256
            at = put(r_.gs_conv, l, at, dot(r_.xeT[:, 0:width], r_.dproj[c, 0:width]))
        put(r_.gs_conv, l, at, dot(r_.efT[...], r_.dce[...]))

    def back_input(l):
        dx = r_.dxo[...]
        dx = dx + r_.dxs[l, z, par].astype(F32)
        for slot in range(3):
            arrive(r_.ro.at[l, slot], r_.ro_r.at[l, slot])
            dx = dx + r_.ro[l, slot].astype(F32)
        for t in range(2, NZ):
            c = z_from(t)
            arrive(r_.rs2.at[l, c], r_.rsc_r.at[l, t])
            dx = dx + r_.rs2[l, c].astype(F32)
        arrive(r_.hr.at[l, 0], r_.hal_r.at[l, 1])
        arrive(r_.hr.at[l, 1], r_.hal_r.at[l, 0])
        back = jnp.concatenate(
            [r_.hr[l, 0].astype(F32)[0:24], r_.hr[l, 1].astype(F32)[0:24], jnp.zeros((16, D), F32)], 0
        )
        return dx + dot(r_.A[...], back.astype(BF16))

    r_.dy[...] = r_.cot[...].astype(F32)

    E1, C1, Q1, E0, C0, QK0, V0 = range(len(GROUPS))

    def steps(*pairs):
        return [functools.partial(reduce_step, g, k) for g, k in pairs]

    def backward(b, carry):
        l = L - 1 - b
        first, last = b == 0, b == L - 1
        k = 4 + 2 * b
        when(last, *steps((Q1, 1)))
        back_feed_forward(l, k)
        when(last, *steps((C1, 2), (Q1, 2), (E1, 5)))
        back_norms(l, k)
        when(first, *steps((E1, 0)))
        when(last, *steps((E0, 0), (C1, 3), (Q1, 3)), functools.partial(back_convolution, l),
             functools.partial(conv_weight_grads, l), *steps((C0, 0), (E0, 1), (C1, 4), (Q1, 4)))

        def between(i, hf):
            when(first & (i == 0) & (hf == 1), *steps((E1, 1)))
            when(first & (i == 1) & (hf == 1), *steps((E1, 3)))
            when(last & (i == 0) & (hf == 0), *steps((C0, 1), (E0, 2)))
            when(last & (i == 0) & (hf == 1), *steps((C1, 5), (Q1, 5), (E1, 6)))
            when(last & (i == 1) & (hf == 0), *steps((C0, 2), (E0, 3)))
            when(last & (i == 1) & (hf == 1), *steps((C0, 3), (C1, 6), (Q1, 6)))
            for t in range(2, NZ):
                when((i == 1) & (hf == 0), functools.partial(pass_on, l, 0, t))

        def block(i, carry):
            back_attention_block(l, i, between)
            when(first & (i == 0), functools.partial(back_convolution, l), *steps((E1, 2)))
            return carry

        lax.fori_loop(0, NB, block, 0)
        dqb = (r_.dq[...] * scale).astype(BF16)
        r_.dxo[...] += dot_nt(dqb, r_.wqkv[l, :, 0:D])
        when(first, functools.partial(conv_weight_grads, l), *steps((C1, 0)))
        at = put(r_.gs_qkv, l, 0, dot(r_.xeT[:, 0:R], dqb))
        put(r_.gs_qkv, l, at, r_.gkv[...].T)
        when(last, *steps((QK0, 0), (V0, 0), (E0, 4)))
        dx = back_input(l)
        r_.dy[...] = dx

        @pl.when(first)
        def _():
            below = L - 2
            zero_row = jnp.zeros((1, D), F32)
            sync_start(5, pack(col_sum(dx), col_sum(dx * r_.z2[below]), zero_row, zero_row))
            for step in steps((C1, 1), (Q1, 0), (E1, 4)):
                step()
            s2, g2, _, _ = sync_finish(5, combine_sum)
            r_.gshift[below, 2:3] = s2
            r_.ggain[below, 2:3] = g2

        return carry

    lax.fori_loop(0, L, backward, 0)
    in_copy = pltpu.make_async_copy(r_.dy, r_.grad_in, r_.store.at[1])
    in_copy.start()
    for step in steps(
        (V0, 1), (QK0, 1), (C0, 4), (E0, 5),
        (V0, 2), (QK0, 2), (C0, 5), (E0, 6),
        (V0, 3), (QK0, 3), (C0, 6),
        (V0, 4), (QK0, 4),
    ):
        step()
    for l in range(L):
        for k in range(3):
            r_.ggain_out[k, l : l + 1] = r_.ggain[l, k : k + 1]
            r_.gshift_out[k, l : l + 1] = r_.gshift[l, k : k + 1]
    for g in range(len(GROUPS)):
        reduce_drain(g)
    sent(r_.meta.at[0 : N - 1], r_.meta_s.at[0])
    for k in range(SYNCS):
        sent(r_.st1.at[k, 0 : M * N - 1], r_.st1_s.at[k])
    for l in range(L):
        for t in range(NZ):
            sent(r_.gb.at[l, 0], r_.agp_s.at[l, t])
            if t > 0:
                sent(r_.gb.at[l, 0], r_.agc_s.at[l, t])
            if t > 1:
                sent(r_.rs1.at[l, 0], r_.rsc_s.at[l, t])
        for slot in range(2 * (NB - 1)):
            sent(r_.rs1.at[l, 0], r_.rsp_s.at[l, slot])
        for slot in range(3):
            sent(r_.ro.at[l, 0], r_.ro_s.at[l, slot])
        for side in range(2):
            sent(r_.hs.at[l, 0], r_.hal_s.at[l, side])
    act_copy.wait()
    in_copy.wait()


def finish_kernel(act_h, gin_h, *refs):
    n = len(GROUPS)
    held, (ggain_h, gshift_h), refs = refs[:n], refs[n : n + 2], refs[n + 2 :]
    act_o, gin_o, proj_o, edge_o, qkv_o, out_o, up_o, down_o, ggain_o, gshift_o = refs[:10]
    summed, refs = refs[10 : 10 + n], refs[10 + n :]
    act, gin, proj, edge, qkv, out, up, down, in_sem, out_sem = refs
    loads = [
        pltpu.make_async_copy(src, dst, in_sem.at[i])
        for i, (src, dst) in enumerate(zip(held + (act_h, gin_h), summed + (act, gin), strict=True))
    ]
    for load in loads:
        load.start()
    ggain_o[...] = ggain_h[...]
    gshift_o[...] = gshift_h[...]
    stores = []

    def store(src, dst):
        copy = pltpu.make_async_copy(src, dst, out_sem.at[len(stores)])
        copy.start()
        stores.append(copy)

    def widen(dst, l, g, at, first=0, last=None):
        rows = dst.shape[1]
        for c in range(first, dst.shape[2] // 128 if last is None else last):
            dst[l, :, 128 * c : 128 * (c + 1)] = summed[g][at : at + rows].astype(F32)
            at += rows
        return at

    for g, (name, l, first, rows, _) in enumerate(GROUPS):
        loads[g].wait()
        if name == "early":
            at = widen(out, l, g, 0)
            store(out.at[l], out_o.at[l])
            at = widen(up, l, g, at)
            store(up.at[l], up_o.at[l])
            widen(down, l, g, at)
            store(down.at[l], down_o.at[l])
        elif name == "conv":
            at = widen(proj, l, g, 0)
            store(proj.at[l], proj_o.at[l])
            widen(edge, l, g, at)
            store(edge.at[l], edge_o.at[l])
        else:
            widen(qkv, l, g, 0, first // 256, (first + rows) // 256)
            if first + rows == 1536:
                store(qkv.at[l], qkv_o.at[l])
    for i, (src, dst) in enumerate(((act, act_o), (gin, gin_o))):
        loads[n + i].wait()
        store(src, dst)
    for copy in stores:
        copy.wait()


def fused_device(
    N, M, node_input, edge_feat, graph_ids, edge_src, edge_dst, halo_send, w_proj, w_edge, w_qkv,
    w_out, w_up, w_down, norm_gain, norm_shift, cotangent,
):
    R, D = node_input.shape
    E = edge_feat.shape[0]
    L = w_proj.shape[0]
    names = scratch_list(N, M, L, R, E)
    vmem = pl.BlockSpec(memory_space=pltpu.VMEM)
    hbm = pl.BlockSpec(memory_space=pltpu.HBM)
    shape = jax.ShapeDtypeStruct
    rows = shape((R, D), F32)
    norm = shape((3, L, D), F32)
    groups = [shape((rows_g, 128), BF16) for _, _, _, rows_g, _ in GROUPS]
    outs = pl.pallas_call(
        functools.partial(kernel, N, M, L, tuple(names)),
        out_shape=[rows, rows, *groups, norm, norm],
        in_specs=[hbm] + [vmem] * 4 + [hbm] * 7 + [vmem] * 2 + [hbm],
        out_specs=[hbm] * (2 + len(GROUPS)) + [vmem] * 2,
        scratch_shapes=list(names.values()),
        compiler_params=pltpu.CompilerParams(
            collective_id=0, has_side_effects=True, vmem_limit_bytes=60 << 20
        ),
        name="layers",
    )(node_input, graph_ids, edge_src, edge_dst, halo_send, edge_feat, w_proj, w_edge, w_qkv, w_out, w_up,
      w_down, norm_gain.transpose(1, 0, 2), norm_shift.transpose(1, 0, 2), cotangent)
    weights = [shape(w.shape, F32) for w in (w_proj, w_edge, w_qkv, w_out, w_up, w_down)]
    results = pl.pallas_call(
        finish_kernel,
        out_shape=[rows, rows, *weights, norm, norm],
        in_specs=[hbm] * (2 + len(GROUPS)) + [vmem] * 2,
        out_specs=[hbm] * 8 + [vmem] * 2,
        scratch_shapes=[pltpu.VMEM(s.shape, s.dtype) for s in (*groups, rows, rows, *weights)]
        + [pltpu.SemaphoreType.DMA((len(GROUPS) + 2,)), pltpu.SemaphoreType.DMA((14,))],
        compiler_params=pltpu.CompilerParams(vmem_limit_bytes=60 << 20),
        name="gradients",
    )(*outs)
    ggain, gshift = results[8].transpose(1, 0, 2), results[9].transpose(1, 0, 2)
    return (*results[:8], ggain, gshift)


BLOCK_CAP = 2048


def extended_2(block, sides, width):
    for axis, dim in sides:
        count = lax.axis_size(axis)
        forward = [(i, i + 1) for i in range(count - 1)]
        forward.append((count - 1, 0))
        backward = [(target, source) for source, target in forward]
        low = lax.ppermute(
            lax.slice_in_dim(block, block.shape[dim] - width, None, axis=dim), axis, forward
        )
        high = lax.ppermute(lax.slice_in_dim(block, 0, width, axis=dim), axis, backward)
        block = jnp.concatenate([low, block, high], axis=dim)
    return block


def block_length(total_rows, upper_limit):
    for length in range(min(total_rows, upper_limit), 0, -1):
        if total_rows % length == 0:
            return length
    return 1


def outer_product(left, right):
    return lax.dot_general(
        left, right, (((0,), (0,)), ((), ())), preferred_element_type=jnp.float32
    )


def times_transposed(left, weight):
    return lax.dot_general(
        left, weight, (((1,), (1,)), ((), ())), preferred_element_type=jnp.float32
    )


def forward_product(left, weight):
    return jnp.dot(left, weight, preferred_element_type=jnp.float32)


def silu_slope_plain(inputs):
    logistic = jax.nn.sigmoid(inputs)
    return logistic * (1.0 + inputs * (1.0 - logistic))


def normalize(inputs, gain_row, shift_row, node_total):
    batch_mean = lax.psum(jnp.sum(inputs, 0), ("nodes", "rep")) / node_total
    centred = inputs - batch_mean
    batch_var = lax.psum(jnp.sum(centred * centred, 0), ("nodes", "rep")) / node_total
    inv_std = lax.rsqrt(batch_var + NORM_EPS)
    standard = (inputs - batch_mean) * inv_std
    return (standard * gain_row + shift_row, standard, inv_std)


def normalize_back(grad_out, standard, inv_std, gain_row, node_total):
    shift_grad, gain_grad = lax.psum(
        (jnp.sum(grad_out, 0), jnp.sum(grad_out * standard, 0)), ("nodes", "rep")
    )
    grad_in = (
        gain_row
        * inv_std
        * (grad_out - shift_grad / node_total - standard * gain_grad / node_total)
    )
    return (grad_in, gain_grad, shift_grad)


def exchange_sources(outgoing):
    halo_rows = outgoing.shape[0] // 2
    grown = extended_2(outgoing, (("nodes", 0),), halo_rows)
    return jnp.concatenate([grown[:halo_rows], grown[3 * halo_rows :]], 0)


def return_sources(incoming_grad):
    halo_rows = incoming_grad.shape[0] // 2
    grown = extended_2(incoming_grad.astype(jnp.bfloat16), (("nodes", 0),), halo_rows).astype(
        incoming_grad.dtype
    )
    return jnp.concatenate([grown[:halo_rows], grown[3 * halo_rows :]], 0)


def attend_forward(query_rows, key_rows, value_rows, local_graphs, group_graphs):
    row_count = query_rows.shape[0]
    score_scale = HEAD_DIM ** (-0.5)
    queries = query_rows.reshape(row_count, HEADS, HEAD_DIM)

    def add_piece(carried, kv_piece, first_row):
        key_piece, value_piece = kv_piece
        piece_rows = key_piece.shape[0]
        block_len = block_length(piece_rows, BLOCK_CAP)

        def add_block(block_state, block_index):
            row_max, row_sum, accumulated = block_state
            block_start = block_index * block_len
            key_block = lax.dynamic_slice_in_dim(key_piece, block_start, block_len, 0).reshape(
                block_len, HEADS, HEAD_DIM
            )
            value_block = lax.dynamic_slice_in_dim(value_piece, block_start, block_len, 0).reshape(
                block_len, HEADS, HEAD_DIM
            )
            key_graphs = lax.dynamic_slice_in_dim(
                group_graphs, first_row + block_start, block_len, 0
            )
            same_graph = (local_graphs[:, None] == key_graphs[None, :])[None]
            scores = (
                jnp.einsum("qhd,khd->hqk", queries, key_block, preferred_element_type=jnp.float32)
                * score_scale
            )
            scores = jnp.where(same_graph, scores, NEG)
            new_max = jnp.maximum(row_max, jnp.max(scores, 2))
            weights = jnp.where(same_graph, jnp.exp(scores - new_max[:, :, None]), 0.0)
            factor = jnp.exp(row_max - new_max)
            row_sum = row_sum * factor + jnp.sum(weights, 2)
            contrib = jnp.einsum(
                "hqk,khd->qhd",
                weights.astype(jnp.bfloat16),
                value_block,
                preferred_element_type=jnp.float32,
            )
            accumulated = accumulated * jnp.transpose(factor)[:, :, None] + contrib
            return ((new_max, row_sum, accumulated), None)

        carried, _ = lax.scan(add_block, carried, jnp.arange(piece_rows // block_len))
        return carried

    start_state = (
        jnp.full((HEADS, row_count), NEG, jnp.float32),
        jnp.zeros((HEADS, row_count), jnp.float32),
        jnp.zeros((row_count, HEADS, HEAD_DIM), jnp.float32),
    )
    row_max, row_sum, accumulated = add_piece(
        start_state,
        (
            lax.all_gather(key_rows, "nodes", axis=0, tiled=True),
            lax.all_gather(value_rows, "nodes", axis=0, tiled=True),
        ),
        jnp.int32(0),
    )
    attn_raw = accumulated / jnp.transpose(row_sum)[:, :, None]
    log_sum = row_max + jnp.log(row_sum)
    return (attn_raw, log_sum)


def attend_backward(
    query_rows, key_rows, value_rows, grad_low, attn_raw, log_sum, local_graphs, group_graphs
):
    row_count = query_rows.shape[0]
    model_width = HEADS * HEAD_DIM
    score_scale = HEAD_DIM ** (-0.5)
    queries = query_rows.reshape(row_count, HEADS, HEAD_DIM)
    grad_heads = grad_low.reshape(row_count, HEADS, HEAD_DIM)
    row_delta = jnp.einsum("qhd,qhd->hq", grad_heads.astype(jnp.float32), attn_raw)

    def score_block(key_block, value_block, key_graphs):
        same_graph = (local_graphs[:, None] == key_graphs[None, :])[None]
        scores = (
            jnp.einsum("qhd,khd->hqk", queries, key_block, preferred_element_type=jnp.float32)
            * score_scale
        )
        attn_weights = jnp.exp(jnp.where(same_graph, scores - log_sum[:, :, None], NEG))
        grad_weights = jnp.einsum(
            "qhd,khd->hqk", grad_heads, value_block, preferred_element_type=jnp.float32
        )
        grad_scores = (attn_weights * (grad_weights - row_delta[:, :, None])).astype(jnp.bfloat16)
        return (attn_weights, grad_scores)

    def key_terms(attn_weights, grad_scores, block_len):
        grad_keys = (
            jnp.einsum("hqk,qhd->khd", grad_scores, queries, preferred_element_type=jnp.float32)
            * score_scale
        )
        grad_values = jnp.einsum(
            "hqk,qhd->khd",
            attn_weights.astype(jnp.bfloat16),
            grad_heads,
            preferred_element_type=jnp.float32,
        )
        return jnp.concatenate(
            [
                grad_keys.reshape(block_len, model_width),
                grad_values.reshape(block_len, model_width),
            ],
            1,
        )

    def query_term(grad_scores, key_block):
        return (
            jnp.einsum("hqk,khd->qhd", grad_scores, key_block, preferred_element_type=jnp.float32)
            * score_scale
        )

    group_rows = group_graphs.shape[0]

    def add_piece(carried, kv_piece, first_row):
        key_piece, value_piece = kv_piece
        piece_rows = key_piece.shape[0]
        block_len = block_length(piece_rows, BLOCK_CAP)

        def add_block(block_state, block_index):
            grad_query, buffer = block_state
            block_start = block_index * block_len
            key_block = lax.dynamic_slice_in_dim(key_piece, block_start, block_len, 0).reshape(
                block_len, HEADS, HEAD_DIM
            )
            value_block = lax.dynamic_slice_in_dim(value_piece, block_start, block_len, 0).reshape(
                block_len, HEADS, HEAD_DIM
            )
            place = first_row + block_start
            key_graphs = lax.dynamic_slice_in_dim(group_graphs, place, block_len, 0)
            attn_weights, grad_scores = score_block(key_block, value_block, key_graphs)
            grad_query = grad_query + query_term(grad_scores, key_block)
            block_terms = key_terms(attn_weights, grad_scores, block_len)
            current = lax.dynamic_slice_in_dim(buffer, place, block_len, 0)
            buffer = lax.dynamic_update_slice_in_dim(buffer, current + block_terms, place, 0)
            return ((grad_query, buffer), None)

        carried, _ = lax.scan(add_block, carried, jnp.arange(piece_rows // block_len))
        return carried

    start_state = (
        jnp.zeros((row_count, HEADS, HEAD_DIM), jnp.float32),
        jnp.zeros((group_rows, 2 * model_width), jnp.float32),
    )
    grad_query, buffer = add_piece(
        start_state,
        (
            lax.all_gather(key_rows, "nodes", axis=0, tiled=True),
            lax.all_gather(value_rows, "nodes", axis=0, tiled=True),
        ),
        jnp.int32(0),
    )
    grad_kv = lax.psum_scatter(buffer, "nodes", scatter_dimension=0, tiled=True)
    return (
        grad_query.reshape(row_count, model_width),
        grad_kv[:, :model_width],
        grad_kv[:, model_width:],
    )


def layer_forward(
    hidden, params, edge_feat, edge_src, edge_dst, halo_send, local_graphs, group_graphs, node_total
):
    w_proj, w_edge, w_qkv, w_out, w_up, w_down, norm_gains, norm_shifts = params
    row_count, model_width = hidden.shape
    hidden_low = hidden.astype(jnp.bfloat16)
    projected = forward_product(hidden_low, w_proj)
    self_term = projected[:, :model_width]
    dest_term = projected[:, 2 * model_width : 3 * model_width]
    source_rows = jnp.concatenate(
        [projected[:, model_width : 2 * model_width], projected[:, 3 * model_width :]], 1
    ).astype(jnp.bfloat16)
    incoming = exchange_sources(source_rows[halo_send])
    extended = jnp.concatenate([source_rows, incoming], 0)
    edge_rows = extended[edge_src].astype(jnp.float32)
    source_b = edge_rows[:, :model_width]
    source_e = edge_rows[:, model_width:]
    edge_proj = forward_product(edge_feat, w_edge)
    gating = jax.nn.sigmoid(dest_term[edge_dst] + source_e + edge_proj)
    numerator = jax.ops.segment_sum(gating * source_b, edge_dst, row_count)
    denominator = jax.ops.segment_sum(gating, edge_dst, row_count)
    message = self_term + numerator / (denominator + GATE_EPS)
    normed_one, standard_one, inv_one = normalize(
        message, norm_gains[0], norm_shifts[0], node_total
    )
    local_out = hidden + jax.nn.silu(normed_one)
    qkv_low = forward_product(hidden_low, w_qkv).astype(jnp.bfloat16)
    query_rows = qkv_low[:, :model_width]
    key_rows = qkv_low[:, model_width : 2 * model_width]
    value_rows = qkv_low[:, 2 * model_width :]
    attn_raw, log_sum = attend_forward(query_rows, key_rows, value_rows, local_graphs, group_graphs)
    attn_low = attn_raw.reshape(row_count, model_width).astype(jnp.bfloat16)
    attn_proj = forward_product(attn_low, w_out)
    normed_two, standard_two, inv_two = normalize(
        hidden + attn_proj, norm_gains[1], norm_shifts[1], node_total
    )
    mixed = local_out + normed_two
    mixed_low = mixed.astype(jnp.bfloat16)
    up_proj = forward_product(mixed_low, w_up)
    activated = jax.nn.silu(up_proj).astype(jnp.bfloat16)
    down_proj = forward_product(activated, w_down)
    normed_three, standard_three, inv_three = normalize(
        mixed + down_proj, norm_gains[2], norm_shifts[2], node_total
    )
    saved = (
        hidden_low,
        source_b,
        gating,
        numerator,
        denominator,
        normed_one,
        standard_one,
        inv_one,
        query_rows,
        key_rows,
        value_rows,
        attn_raw,
        log_sum,
        attn_low,
        standard_two,
        inv_two,
        mixed_low,
        up_proj,
        activated,
        standard_three,
        inv_three,
    )
    return (normed_three, saved)


def layer_backward(
    grad_out,
    params,
    saved,
    edge_feat,
    edge_src,
    edge_dst,
    halo_send,
    local_graphs,
    group_graphs,
    node_total,
):
    w_proj, w_edge, w_qkv, w_out, w_up, w_down, norm_gains, norm_shifts = params
    (
        hidden_low,
        source_b,
        gating,
        numerator,
        denominator,
        normed_one,
        standard_one,
        inv_one,
        query_rows,
        key_rows,
        value_rows,
        attn_raw,
        log_sum,
        attn_low,
        standard_two,
        inv_two,
        mixed_low,
        up_proj,
        activated,
        standard_three,
        inv_three,
    ) = saved
    row_count, model_width = grad_out.shape
    grad_three, gain_three, shift_three = normalize_back(
        grad_out, standard_three, inv_three, norm_gains[2], node_total
    )
    down_grad = grad_three.astype(jnp.bfloat16)
    grad_w_down = outer_product(activated, down_grad)
    up_grad = (times_transposed(down_grad, w_down) * silu_slope_plain(up_proj)).astype(jnp.bfloat16)
    grad_w_up = outer_product(mixed_low, up_grad)
    grad_mixed = grad_three + times_transposed(up_grad, w_up)
    grad_two, gain_two, shift_two = normalize_back(
        grad_mixed, standard_two, inv_two, norm_gains[1], node_total
    )
    out_grad = grad_two.astype(jnp.bfloat16)
    grad_w_out = outer_product(attn_low, out_grad)
    attn_grad = times_transposed(out_grad, w_out).astype(jnp.bfloat16)
    grad_query, grad_key, grad_value = attend_backward(
        query_rows, key_rows, value_rows, attn_grad, attn_raw, log_sum, local_graphs, group_graphs
    )
    qkv_grad = jnp.concatenate([grad_query, grad_key, grad_value], 1).astype(jnp.bfloat16)
    grad_w_qkv = outer_product(hidden_low, qkv_grad)
    grad_message, gain_one, shift_one = normalize_back(
        grad_mixed * silu_slope_plain(normed_one), standard_one, inv_one, norm_gains[0], node_total
    )
    shifted = denominator + GATE_EPS
    grad_numer = grad_message / shifted
    grad_denom = -grad_message * numerator / (shifted * shifted)
    numer_edge = grad_numer[edge_dst]
    grad_gate = numer_edge * source_b + grad_denom[edge_dst]
    grad_pre_edge = grad_gate * gating * (1.0 - gating)
    edge_grad = grad_pre_edge.astype(jnp.bfloat16)
    grad_w_edge = outer_product(edge_feat, edge_grad)
    grad_dest = jax.ops.segment_sum(grad_pre_edge, edge_dst, row_count)
    grad_extended = jax.ops.segment_sum(
        jnp.concatenate([numer_edge * gating, grad_pre_edge], 1),
        edge_src,
        row_count + halo_send.shape[0],
    )
    returned = return_sources(grad_extended[row_count:])
    grad_source = grad_extended[:row_count].at[halo_send].add(returned)
    proj_grad = jnp.concatenate(
        [grad_message, grad_source[:, :model_width], grad_dest, grad_source[:, model_width:]], 1
    ).astype(jnp.bfloat16)
    grad_w_proj = outer_product(hidden_low, proj_grad)
    grad_hidden = (
        grad_mixed
        + grad_two
        + times_transposed(proj_grad, w_proj)
        + times_transposed(qkv_grad, w_qkv)
    )
    weight_grads = (grad_w_proj, grad_w_edge, grad_w_qkv, grad_w_out, grad_w_up, grad_w_down)
    return (
        grad_hidden,
        weight_grads,
        jnp.stack([gain_one, gain_two, gain_three]),
        jnp.stack([shift_one, shift_two, shift_three]),
    )


def per_device(
    node_input,
    edge_feat,
    graph_ids,
    edge_src,
    edge_dst,
    halo_send,
    w_proj,
    w_edge,
    w_qkv,
    w_out,
    w_up,
    w_down,
    norm_gain,
    norm_shift,
    cotangent,
):
    group_graphs = lax.all_gather(graph_ids, "nodes", axis=0, tiled=True)
    node_total = node_input.shape[0] * lax.axis_size("nodes") * lax.axis_size("rep")
    layer_count = w_proj.shape[0]
    layer_params = [
        (
            w_proj[layer_index],
            w_edge[layer_index],
            w_qkv[layer_index],
            w_out[layer_index],
            w_up[layer_index],
            w_down[layer_index],
            norm_gain[layer_index],
            norm_shift[layer_index],
        )
        for layer_index in range(layer_count)
    ]
    hidden = node_input.astype(jnp.float32)
    saved_all = []
    for layer_index in range(layer_count):
        hidden, saved = layer_forward(
            hidden,
            layer_params[layer_index],
            edge_feat,
            edge_src,
            edge_dst,
            halo_send,
            graph_ids,
            group_graphs,
            node_total,
        )
        saved_all.append(saved)
    grad_hidden = cotangent.astype(jnp.float32)
    weight_parts = [None] * layer_count
    gain_parts = [None] * layer_count
    shift_parts = [None] * layer_count
    for layer_index in range(layer_count - 1, -1, -1):
        (
            grad_hidden,
            weight_parts[layer_index],
            gain_parts[layer_index],
            shift_parts[layer_index],
        ) = layer_backward(
            grad_hidden,
            layer_params[layer_index],
            saved_all[layer_index],
            edge_feat,
            edge_src,
            edge_dst,
            halo_send,
            graph_ids,
            group_graphs,
            node_total,
        )
    proj_local = jnp.stack([weight_parts[layer_index][0] for layer_index in range(layer_count)])
    edge_local = jnp.stack([weight_parts[layer_index][1] for layer_index in range(layer_count)])
    qkv_local = jnp.stack([weight_parts[layer_index][2] for layer_index in range(layer_count)])
    out_local = jnp.stack([weight_parts[layer_index][3] for layer_index in range(layer_count)])
    up_local = jnp.stack([weight_parts[layer_index][4] for layer_index in range(layer_count)])
    down_local = jnp.stack([weight_parts[layer_index][5] for layer_index in range(layer_count)])
    grad_proj, grad_edge, grad_qkv, grad_out, grad_up, grad_down = lax.psum(
        (proj_local, edge_local, qkv_local, out_local, up_local, down_local), ("nodes", "rep")
    )
    return (
        hidden,
        grad_hidden,
        grad_proj,
        grad_edge,
        grad_qkv,
        grad_out,
        grad_up,
        grad_down,
        jnp.stack(gain_parts),
        jnp.stack(shift_parts),
    )


def solution(mesh):
    in_specs = (
        P(("rep", "nodes"), None),
        P(("rep", "nodes"), None),
        P(("rep", "nodes")),
        P(("rep", "nodes")),
        P(("rep", "nodes")),
        P(("rep", "nodes")),
        P(),
        P(),
        P(),
        P(),
        P(),
        P(),
        P(),
        P(),
        P(("rep", "nodes"), None),
    )
    out_specs = (
        P(("rep", "nodes"), None),
        P(("rep", "nodes"), None),
        P(),
        P(),
        P(),
        P(),
        P(),
        P(),
        P(),
        P(),
    )
    N, M = mesh.shape["nodes"], mesh.shape["rep"]
    fused = N in (4, 8) and M % 2 == 0 and 512 % (16 * N * M) == 0
    return jax.shard_map(
        functools.partial(fused_device, N, M) if fused else per_device,
        mesh=mesh, in_specs=in_specs, out_specs=out_specs, check_vma=False,
    )
```

```python
import functools
import math

import jax
import jax.numpy as jnp
from jax import lax
from jax.experimental import pallas as pl
from jax.experimental.pallas import tpu as pltpu
from jax.sharding import PartitionSpec as P

HEADS = 8
HEAD_DIM = 32
NEG = -1e30
NORM_EPS = 1e-05
GATE_EPS = 1e-06
F32, BF16, I32 = jnp.float32, jnp.bfloat16, jnp.int32
MESH = pl.DeviceIdType.MESH
SYNCS = 7
GROUPS = (
    ("early", 1, 0, 2560, ("core", "y", "x", "z")),
    ("conv", 1, 0, 2560, ("core", "y", "x", "z")),
    ("qkv", 1, 0, 1536, ("core", "y", "x", "z")),
    ("early", 0, 0, 2560, ("core", "y", "x", "z")),
    ("conv", 0, 0, 2560, ("core", "y", "x", "z")),
    ("qkv", 0, 0, 1024, ("rep", "nodes")),
    ("qkv", 0, 1024, 512, ("nodes", "rep")),
)


def dot(left, right):
    return lax.dot_general(
        left, right, (((1,), (0,)), ((), ())), preferred_element_type=F32
    )


def dot_nt(left, right):
    return lax.dot_general(
        left, right, (((1,), (1,)), ((), ())), preferred_element_type=F32
    )


def dot_tn(left, right):
    return lax.dot_general(
        left, right, (((0,), (0,)), ((), ())), preferred_element_type=F32
    )


def split(value):
    high = value.astype(BF16)
    return high, (value - high.astype(F32)).astype(BF16)


def select_rows(onehot, value):
    high, low = split(value)
    return dot(onehot, high) + dot(onehot, low)


def sigmoid(value):
    return 1.0 / (1.0 + jnp.exp(-value))


def silu_slope(value):
    logistic = sigmoid(value)
    return logistic * (1.0 + value * (1.0 - logistic))


def col_sum(value):
    return jnp.sum(value, axis=0, keepdims=True)


def pack(first, second, third, fourth):
    halves = []
    for row in (first, second, third, fourth):
        halves += [row[:, :128], row[:, 128:]]
    return jnp.concatenate(halves, 0)


def unpack(tile):
    return [
        jnp.concatenate([tile[2 * i : 2 * i + 1], tile[2 * i + 1 : 2 * i + 2]], 1)
        for i in range(4)
    ]


def combine_pair(tiles, count):
    mean = jnp.mean(tiles[:, 0:4], 0)
    off = tiles[:, 0:4] - mean
    return jnp.concatenate([mean, jnp.sum(tiles[:, 4:8] + count * off * off, 0)], 0)


def combine_last(tiles, count):
    mean = jnp.mean(tiles[:, 0:2], 0)
    off = tiles[:, 0:2] - mean
    return jnp.concatenate(
        [
            mean,
            jnp.sum(tiles[:, 2:4], 0),
            jnp.sum(tiles[:, 4:6] + count * off * off, 0),
            jnp.sum(tiles[:, 6:8] + off * tiles[:, 2:4], 0),
        ],
        0,
    )


def combine_sum(tiles, count):
    return jnp.sum(tiles, 0)


class Refs:
    pass


def axis_sizes(N, M):
    return dict(core=2, y=M // 2, x=2, z=N // 2, rep=M, nodes=N)


def scratch_list(N, M, L, R, E):
    NZ, NB, G = N // 2, N // 4, N * R
    D, FF, W, HH = 256, 512, 4 * R, HEADS // 2 * R
    dma = lambda *shape: pltpu.SemaphoreType.DMA(shape)
    vm = lambda dtype, *shape: pltpu.VMEM(shape, dtype)
    names = dict(
        gb=vm(BF16, L, N, R, D),
        xs=vm(BF16, L, N, R, D),
        meta=vm(I32, N, 8, 256),
        ef=vm(BF16, E, D),
        cot=vm(BF16, R, D),
        wp=vm(BF16, L, D, 4 * D),
        we=vm(BF16, L, D, D),
        wqkv=vm(BF16, L, D, 3 * D),
        wo=vm(BF16, L, D, D),
        wu=vm(BF16, L, D, FF),
        wd=vm(BF16, L, FF, D),
        st1=vm(F32, SYNCS, M * N, 8, 128),
        gain=vm(F32, L, 8, D),
        shift=vm(F32, L, 8, D),
        ggain=vm(F32, L, 8, D),
        gshift=vm(F32, L, 8, D),
        iv=vm(F32, L, 8, D),
        moff=vm(F32, N, 8, D),
        move=vm(F32, 8, D),
        T=vm(BF16, E, R),
        TT=vm(BF16, R, E),
        S=vm(BF16, E, 256),
        ST=vm(BF16, 256, E),
        efT=vm(BF16, D, E),
        HP=vm(BF16, 32, R),
        HN=vm(BF16, 32, R),
        A=vm(BF16, R, 64),
        bias=vm(F32, R, G),
        ce=vm(F32, L, E, D),
        xf=vm(F32, L + 1, R, D),
        xe=vm(BF16, L, 256, D),
        xeT=vm(BF16, D, 256),
        gate=vm(F32, L, E, D),
        bs=vm(BF16, L, E, D),
        num=vm(F32, L, R, D),
        den=vm(F32, L, R, D),
        z0=vm(F32, L, R, D),
        z1=vm(F32, L, R, D),
        z2=vm(F32, L, R, D),
        kk=vm(BF16, L, G, D),
        vv=vm(BF16, L, G, D),
        kT=vm(BF16, D, G),
        vT=vm(BF16, D, G),
        od=vm(F32, NB, R, D),
        md=vm(F32, NB, R, D),
        ld=vm(F32, NB, R, D),
        rb=vm(F32, L, NB, R, D),
        pst=vm(BF16, L, HEADS * R, G),
        oraw=vm(F32, L, R, D),
        ob=vm(BF16, L, R, D),
        mb=vm(BF16, L, R, D),
        u=vm(F32, L, R, FF),
        g=vm(BF16, L, R, FF),
        dy=vm(F32, R, D),
        dmix=vm(F32, R, D),
        dxo=vm(F32, R, D),
        dob=vm(F32, R, D),
        dq=vm(F32, R, D),
        qm=vm(BF16, L, 2, HH, 128),
        qmT=vm(BF16, 2, 128, HH),
        dom=vm(BF16, HH, 128),
        dss=vm(BF16, HH, W),
        dkv=vm(BF16, 2 * D, W),
        gkv=vm(F32, 2 * D, D),
        dce=vm(BF16, E, D),
        dproj=vm(BF16, 4, 256, D),
        dxs=vm(BF16, L, NZ, 2, R, D),
        rs1=vm(BF16, L, NZ, R, D),
        cs=vm(BF16, L, NZ, R, D),
        rs2=vm(BF16, L, NZ, R, D),
        ro=vm(BF16, L, 3, R, D),
        hs=vm(BF16, L, 2, 32, D),
        hr=vm(BF16, L, 2, 32, D),
    )
    names.update(
        gs_early=vm(BF16, L, 2560, 128),
        gs_conv=vm(BF16, L, 2560, 128),
        gs_qkv=vm(BF16, L, 1536, 128),
    )
    sizes = axis_sizes(N, M)
    for g, (_, _, _, rows, stages) in enumerate(GROUPS):
        names[f"go{g}"] = vm(BF16, rows, 128)
        left = rows
        for k, axis in enumerate(stages):
            left //= sizes[axis]
            names[f"ga{g}_{k}"] = vm(BF16, sizes[axis] - 1, left, 128)
            if k < len(stages) - 1:
                names[f"gh{g}_{k}"] = vm(BF16, left, 128)
    names.update(
        ar_s=dma(len(GROUPS), 8),
        ar_r=dma(len(GROUPS), 8),
        ar_l=dma(len(GROUPS)),
        load=dma(10),
        store=dma(2),
        meta_s=dma(1),
        meta_r=dma(1),
        st1_s=dma(SYNCS),
        st1_r=dma(SYNCS),
        agc_s=dma(L, NZ),
        agc_r=dma(L, NZ),
        agp_s=dma(L, NZ),
        agp_r=dma(L, NZ),
        rsp_s=dma(L, NZ),
        rsp_r=dma(L, NZ),
        ro_s=dma(L, 3),
        ro_r=dma(L, 3),
        rsc_s=dma(L, NZ),
        rsc_r=dma(L, NZ),
        hal_s=dma(L, 2),
        hal_r=dma(L, 2),
    )
    return names


IN_NAMES = (
    "x_in", "ids", "edge_src", "edge_dst", "halo", "ef_h", "wp_h", "we_h", "wqkv_h", "wo_h", "wu_h", "wd_h",
    "gain_in", "shift_in", "cot_h",
)
OUT_NAMES = ("out_act", "grad_in", *(f"gout{g}" for g in range(len(GROUPS))), "ggain_out", "gshift_out")


def kernel(N, M, L, names, *args):
    r_ = Refs()
    for name, ref in zip(IN_NAMES + OUT_NAMES + tuple(names), args, strict=True):
        setattr(r_, name, ref)
    R, D = r_.x_in.shape
    E = r_.ef.shape[0]
    NZ, NB, G, W = N // 2, N // 4, N * R, 4 * R
    HK = HEADS // 2
    total = float(N * M * R)
    scale = HEAD_DIM ** -0.5
    me = lax.axis_index("nodes")
    rep = lax.axis_index("rep")
    z = me // 2
    par = me % 2
    partner = 2 * z + (1 - par)
    prev = (me + N - 1) % N
    nxt = (me + 1) % N
    zh, zl = z // 2, z % 2
    z_to = lambda t: 2 * ((zh + t // 2) % NB) + (zl + t % 2) % 2
    z_from = lambda t: 2 * ((zh + NB - t // 2) % NB) + (zl + t % 2) % 2

    def remote(src, dst, s_sem, r_sem, **where):
        return pltpu.make_async_remote_copy(
            src_ref=src, dst_ref=dst, send_sem=s_sem, recv_sem=r_sem,
            device_id=where, device_id_type=MESH,
        )

    def send(src, dst, s_sem, r_sem, **where):
        remote(src, dst, s_sem, r_sem, **where).start()

    def arrive(dst, r_sem):
        remote(dst, dst, r_sem, r_sem, nodes=partner).wait_recv()

    def sent(src, s_sem):
        remote(src, src, s_sem, s_sem, nodes=partner).wait_send()

    def when(condition, *acts):
        @pl.when(condition)
        def _():
            for act in acts:
                act()

    loads = [
        pltpu.make_async_copy(getattr(r_, f"{name}_h"), getattr(r_, name), r_.load.at[i])
        for i, name in enumerate(("ef", "we", "wqkv", "wp", "wo", "wu", "wd", "cot"))
    ]
    own_rows = pltpu.make_async_copy(r_.x_in, r_.gb.at[0, me], r_.load.at[8])
    own_rows.start()
    for load in loads:
        load.start()

    barrier = pltpu.get_barrier_semaphore()
    for dr in range(M):
        for d in range(N):
            if dr + d > 0:
                pl.semaphore_signal(barrier, inc=1, device_id={"rep": (rep + dr) % M, "nodes": (me + d) % N},
                                    device_id_type=MESH)
    pl.semaphore_wait(barrier, M * N - 1)

    def gather_start(l):
        mine = r_.gb.at[l, me]
        send(mine, mine, r_.agp_s.at[l, 0], r_.agp_r.at[l, 0], nodes=partner)
        send(mine, mine, r_.agc_s.at[l, 1], r_.agc_r.at[l, 1], nodes=2 * z_to(1) + par)
        send(mine, mine, r_.agp_s.at[l, 1], r_.agp_r.at[l, 1], nodes=2 * z_to(1) + 1 - par)
        for t in range(2, NZ):
            send(mine, mine, r_.agc_s.at[l, t], r_.agc_r.at[l, t], nodes=2 * z_to(t) + par)

    def gather_pass(l, t):
        piece = r_.gb.at[l, 2 * z_from(t) + par]
        arrive(piece, r_.agc_r.at[l, t])
        send(piece, piece, r_.agp_s.at[l, t], r_.agp_r.at[l, t], nodes=partner)

    def gather_take(l, t):
        arrive(r_.gb.at[l, 2 * z_from(t) + 1 - par], r_.agp_r.at[l, t])

    def sync_start(k, tile):
        mine = rep * N + me
        r_.st1[k, mine] = tile
        for dr in range(M):
            for d in range(N):
                if dr + d > 0:
                    send(r_.st1.at[k, mine], r_.st1.at[k, mine], r_.st1_s.at[k], r_.st1_r.at[k],
                         rep=(rep + dr) % M, nodes=(me + d) % N)

    def sync_finish(k, combine):
        arrive(r_.st1.at[k, 0 : M * N - 1], r_.st1_r.at[k])
        return unpack(combine(r_.st1[k], float(R)))

    sizes = axis_sizes(N, M)
    core, row = rep % 2, rep // 2
    places = dict(
        core=(core, lambda t: dict(rep=2 * row + t)),
        y=(row, lambda t: dict(rep=2 * t + core)),
        x=(par, lambda t: dict(nodes=2 * z + t)),
        z=(z, lambda t: dict(nodes=2 * t + par)),
        rep=(rep, lambda t: dict(rep=t)),
        nodes=(me, lambda t: dict(nodes=t)),
    )

    def reduce_step(g, step):
        name, layer, first, rows, stages = GROUPS[g]
        K = len(stages)
        gs, out = getattr(r_, f"gs_{name}").at[layer, first : first + rows], getattr(r_, f"go{g}")
        count, offset = [rows], [0]
        for axis in stages:
            count.append(count[-1] // sizes[axis])
            offset.append(offset[-1] + places[axis][0] * count[-1])
        take = lambda start, size: pl.ds(pl.multiple_of(start, 16), size)
        if 1 <= step <= K:
            k = step - 1
            got = getattr(r_, f"ga{g}_{k}")
            arrive(got, r_.ar_r.at[g, k])
            held = gs if k == 0 else getattr(r_, f"gh{g}_{k - 1}")
            index = places[stages[k]][0]
            acc = held[take(index * count[k + 1], count[k + 1])].astype(F32)
            for slot in range(sizes[stages[k]] - 1):
                acc = acc + got[slot].astype(F32)
            if step < K:
                getattr(r_, f"gh{g}_{k}")[...] = acc.astype(BF16)
            else:
                out[take(offset[K], count[K])] = acc.astype(BF16)
        elif step > K:
            k = 2 * K - step
            arrive(out.at[0 : (sizes[stages[k]] - 1) * count[k + 1]], r_.ar_r.at[g, step - 1])
        if step < K:
            held = gs if step == 0 else getattr(r_, f"gh{g}_{step - 1}")
            index, device = places[stages[step]]
            size = sizes[stages[step]]
            for d in range(1, size):
                to = (index + d) % size
                send(held.at[take(to * count[step + 1], count[step + 1])], getattr(r_, f"ga{g}_{step}").at[d - 1],
                     r_.ar_s.at[g, step], r_.ar_r.at[g, step], **device(to))
        elif step < 2 * K:
            k = 2 * K - 1 - step
            index, device = places[stages[k]]
            size = sizes[stages[k]]
            here = out.at[take(offset[k + 1], count[k + 1])]
            for d in range(1, size):
                send(here, here, r_.ar_s.at[g, step], r_.ar_r.at[g, step], **device((index + d) % size))
        else:
            pltpu.make_async_copy(out, getattr(r_, f"gout{g}"), r_.ar_l.at[g]).start()

    def reduce_drain(g):
        _, _, _, rows, stages = GROUPS[g]
        K, left = len(stages), rows
        out = getattr(r_, f"go{g}")
        for k, axis in enumerate(stages):
            left //= sizes[axis]
            for step in (k, 2 * K - 1 - k):
                sent(out.at[0 : (sizes[axis] - 1) * left], r_.ar_s.at[g, step])
        pltpu.make_async_copy(out, getattr(r_, f"gout{g}"), r_.ar_l.at[g]).wait()

    def put(buf, l, at, value):
        rows = value.shape[0]
        for c in range(value.shape[1] // 128):
            buf[l, at : at + rows] = value[:, 128 * c : 128 * (c + 1)].astype(BF16)
            at += rows
        return at

    lane_head = lax.broadcasted_iota(I32, (R, 128), 1) // HEAD_DIM

    def by_head(parts):
        out = parts[0]
        for k in range(1, HK):
            out = jnp.where(lane_head == k, parts[k], out)
        return out

    r_.meta[me] = jnp.full((8, 256), -1, I32)
    r_.meta[me, 0:1, 0:R] = r_.ids[...].reshape(1, R)
    r_.meta[me, 1:2, 0:48] = r_.halo[...].reshape(1, 48)
    for d in range(1, N):
        send(r_.meta.at[me], r_.meta.at[me], r_.meta_s.at[0], r_.meta_r.at[0], nodes=(me + d) % N)
    own_rows.wait()
    gather_start(0)

    src_row = r_.edge_src[...].reshape(1, E)
    src_row = jnp.where(src_row < R + 24, src_row, src_row + 8)
    dst_row = r_.edge_dst[...].reshape(1, E)
    src_col = jnp.broadcast_to(src_row, (128, E)).T[:, 0:1]
    dst_col = jnp.broadcast_to(dst_row, (128, E)).T[:, 0:1]
    as_mask = lambda cond: cond.astype(F32).astype(BF16)
    r_.T[...] = as_mask(dst_col == lax.broadcasted_iota(I32, (E, R), 1))
    r_.TT[...] = as_mask(dst_row == lax.broadcasted_iota(I32, (R, E), 0))
    r_.S[...] = as_mask(src_col == lax.broadcasted_iota(I32, (E, 256), 1))
    r_.ST[...] = as_mask(src_row == lax.broadcasted_iota(I32, (256, E), 0))
    loads[0].wait()
    r_.efT[...] = r_.ef[...].T
    loads[1].wait()
    for l in range(L):
        r_.ce[l] = dot(r_.ef[...], r_.we[l])
        for k in range(3):
            r_.gain[l, k : k + 1] = r_.gain_in[k, l : l + 1]
            r_.shift[l, k : k + 1] = r_.shift_in[k, l : l + 1]
    r_.xf[0] = r_.gb[0, me].astype(F32)
    r_.moff[...] = jnp.zeros((N, 8, D), F32)
    r_.move[0:1] = jnp.ones((1, D), F32)
    r_.move[1:2] = jnp.zeros((1, D), F32)
    for load in loads[2:]:
        load.wait()

    arrive(r_.meta.at[0 : N - 1], r_.meta_r.at[0])
    id_col = jnp.broadcast_to(r_.meta[me][0:1, 0:R], (128, R)).T[:, 0:1]
    id_row = jnp.concatenate([r_.meta[j][0:1, 0:R] for j in range(N)], 1)
    r_.bias[...] = jnp.where(id_col == id_row, 0.0, NEG)

    def halo_onehot(device, start):
        col = jnp.broadcast_to(r_.meta[device][1:2, 0:128], (128, 128)).T[start : start + 24, 0:1]
        hot = (col == lax.broadcasted_iota(I32, (24, R), 1)).astype(F32)
        return jnp.concatenate([hot, jnp.zeros((8, R), F32)], 0).astype(BF16)

    r_.HP[...] = halo_onehot(prev, 24)
    r_.HN[...] = halo_onehot(nxt, 0)
    r_.A[...] = as_mask(r_.meta[me][1:2, 0:64] == lax.broadcasted_iota(I32, (R, 64), 0))

    factor_exp = scale * math.log2(math.e)

    def prepare_queries(l):
        q = dot(r_.xs[l, me], r_.wqkv[l, :, :D]).astype(BF16).astype(F32)
        for hf in range(2):
            for k in range(HK):
                part = jnp.where(lane_head == k, q[:, 128 * hf : 128 * (hf + 1)], 0.0)
                r_.qm[l, hf, k * R : (k + 1) * R] = part.astype(BF16)

    def head_rows(hf, k, count=1):
        return pl.ds(pl.multiple_of((hf * HK + k) * R, 64), count * R)

    def lane_half(hf):
        return pl.ds(pl.multiple_of(hf * 128, 128), 128)

    def attention_block(l, i, middle):
        half = (zh + NB - i) % NB
        rows = pl.ds(pl.multiple_of(half * W, 128), W)
        x = r_.xs[l, pl.ds(4 * half, 4)].reshape(W, D)
        key = dot(x, r_.wqkv[l, :, D : 2 * D]).astype(BF16)
        r_.kk[l, rows] = key
        r_.kT[:, rows] = key.T
        r_.vv[l, rows] = dot(x, r_.wqkv[l, :, 2 * D :]).astype(BF16)

        def heads(hf, carry):
            lanes = lane_half(hf)
            tops, sums, outs = [], [], []
            for c in range(HK // 2):
                scores = dot(r_.qm[l, hf, 2 * c * R : 2 * (c + 1) * R], r_.kT[lanes, rows])
                for k in range(2):
                    s = scores[k * R : (k + 1) * R] + r_.bias[:, rows]
                    top = jnp.max(s, 1, keepdims=True)
                    e = jnp.exp2((s - top) * factor_exp)
                    tops.append(top)
                    sums.append(jnp.sum(e, 1, keepdims=True))
                    r_.pst[l, head_rows(hf, 2 * c + k), rows] = e.astype(BF16)
                o = dot(r_.pst[l, head_rows(hf, 2 * c, 2), rows], r_.vv[l, rows, lanes])
                outs += [o[0:R], o[R : 2 * R]]
            r_.md[i, :, lanes] = by_head([jnp.broadcast_to(v, (R, 128)) for v in tops])
            r_.ld[i, :, lanes] = by_head([jnp.broadcast_to(v, (R, 128)) for v in sums])
            r_.od[i, :, lanes] = by_head(outs)
            middle(i, hf)
            return carry

        lax.fori_loop(0, 2, heads, 0)

    def attention_end(l):
        top = r_.md[0]
        for i in range(1, NB):
            top = jnp.maximum(top, r_.md[i])
        factors = [jnp.exp2((r_.md[i] - top) * factor_exp) for i in range(NB)]
        inv = 1.0 / sum(factors[i] * r_.ld[i] for i in range(NB))
        o = jnp.zeros((R, D), F32)
        for i in range(NB):
            r_.rb[l, i] = factors[i] * inv
            o = o + factors[i] * inv * r_.od[i]
        r_.oraw[l] = o
        ob = o.astype(BF16)
        r_.ob[l] = ob
        t1 = r_.xf[l] + dot(ob, r_.wo[l])
        r_.z1[l] = t1
        mean1 = col_sum(t1) / R
        return mean1, col_sum((t1 - mean1) * (t1 - mean1))

    def convolution(l):
        xs = r_.xs
        xb = xs[l, me]
        r_.xe[l, 0:R] = xb
        r_.xe[l, R : R + 32] = dot(r_.HP[...], xs[l, prev]).astype(BF16)
        r_.xe[l, R + 32 : R + 64] = dot(r_.HN[...], xs[l, nxt]).astype(BF16)
        xe = r_.xe[l]
        tab_b = dot(xe, r_.wp[l, :, D : 2 * D]).astype(BF16)
        tab_e = dot(xe, r_.wp[l, :, 3 * D :]).astype(BF16)
        pa = dot(xb, r_.wp[l, :, 0:D])
        pd = dot(xb, r_.wp[l, :, 2 * D : 3 * D])
        bs = dot(r_.S[...], tab_b)
        r_.bs[l] = bs.astype(BF16)
        gate = sigmoid(select_rows(r_.T[...], pd) + dot(r_.S[...], tab_e) + r_.ce[l])
        r_.gate[l] = gate
        num = select_rows(r_.TT[...], gate * bs)
        den = select_rows(r_.TT[...], gate)
        r_.num[l] = num
        r_.den[l] = den
        msg = pa + num / (den + GATE_EPS)
        r_.z0[l] = msg

    def forward(l, carry):
        def ready(js):
            for j in js:
                moved = (r_.gb[l, j].astype(F32) + r_.moff[j, 0:1]) * r_.move[0:1] + r_.move[1:2]
                r_.xs[l, j] = moved.astype(BF16)

        r_.xs[l, me] = r_.xf[l].astype(BF16)
        prepare_queries(l)
        arrive(r_.gb.at[l, 2 * z_from(1) + par], r_.agc_r.at[l, 1])
        gather_take(l, 0)
        gather_take(l, 1)
        ready([partner, 2 * z_from(1) + par, 2 * z_from(1) + 1 - par])

        def middle(i, hf):
            when((i == 0) & (hf == 0), *[functools.partial(gather_pass, l, t) for t in range(2, NZ)])

        def block(i, carry):
            attention_block(l, i, middle)

            @pl.when(i == 0)
            def _():
                for t in range(2, NZ):
                    gather_take(l, t)
                ready([2 * z_from(t) + p for t in range(2, NZ) for p in range(2)])
                convolution(l)

            return carry

        lax.fori_loop(0, NB, block, 0)
        mean1, sq1 = attention_end(l)
        msg = r_.z0[l]
        mean0 = col_sum(msg) / R
        sq0 = col_sum((msg - mean0) * (msg - mean0))
        sync_start(2 * l, pack(mean0, mean1, sq0, sq1))
        mean0, mean1, sq0, sq1 = sync_finish(2 * l, combine_pair)
        inv0 = lax.rsqrt(sq0 / total + NORM_EPS)
        inv1 = lax.rsqrt(sq1 / total + NORM_EPS)
        r_.iv[l, 0:1] = inv0
        r_.iv[l, 1:2] = inv1
        z0 = (r_.z0[l] - mean0) * inv0
        z1 = (r_.z1[l] - mean1) * inv1
        r_.z0[l] = z0
        r_.z1[l] = z1
        n0 = z0 * r_.gain[l, 0:1] + r_.shift[l, 0:1]
        mix = r_.xf[l] + n0 * sigmoid(n0) + z1 * r_.gain[l, 1:2] + r_.shift[l, 1:2]
        mb = mix.astype(BF16)
        r_.mb[l] = mb
        u = dot(mb, r_.wu[l])
        r_.u[l] = u
        g = (u * sigmoid(u)).astype(BF16)
        r_.g[l] = g
        y = mix + dot(g, r_.wd[l])
        r_.z2[l] = y
        mean = col_sum(y) / R
        cent = y - mean
        k = 2 * l + 1
        dy = r_.cot[...].astype(F32)
        sync_start(k, pack(mean, col_sum(dy), col_sum(cent * cent), col_sum(dy * cent)))

        @pl.when(l < L - 1)
        def _():
            r_.gb[l + 1, me] = cent.astype(BF16)
            gather_start(l + 1)

        tot_mean, dy_sum, tot_sq, dy_cent = sync_finish(k, combine_last)
        inv2 = lax.rsqrt(tot_sq / total + NORM_EPS)
        r_.iv[l, 2:3] = inv2
        z2 = (r_.z2[l] - tot_mean) * inv2
        r_.z2[l] = z2
        gain, shift = r_.gain[l, 2:3], r_.shift[l, 2:3]
        r_.xf[l + 1] = z2 * gain + shift
        r_.gshift[l, 2:3] = dy_sum
        r_.ggain[l, 2:3] = dy_cent * inv2
        for j in range(N):
            tile = r_.st1[k, rep * N + j]
            r_.moff[j, 0:1] = jnp.concatenate([tile[0:1], tile[1:2]], 1) - tot_mean
        r_.move[0:1] = inv2 * gain
        r_.move[1:2] = shift
        return carry

    lax.fori_loop(0, L, forward, 0)
    act_copy = pltpu.make_async_copy(r_.xf.at[L], r_.out_act, r_.store.at[0])
    act_copy.start()

    def back_feed_forward(l, k):
        s2, g2 = r_.gshift[l, 2:3], r_.ggain[l, 2:3]
        d3 = r_.gain[l, 2:3] * r_.iv[l, 2:3] * (r_.dy[...] - s2 / total - r_.z2[l] * (g2 / total))
        db = d3.astype(BF16)
        dub = (dot_nt(db, r_.wd[l]) * silu_slope(r_.u[l])).astype(BF16)
        dmix = d3 + dot_nt(dub, r_.wu[l])
        r_.dmix[...] = dmix
        n0 = r_.z0[l] * r_.gain[l, 0:1] + r_.shift[l, 0:1]
        gy0 = dmix * silu_slope(n0)
        sync_start(k, pack(col_sum(dmix), col_sum(dmix * r_.z1[l]), col_sum(gy0), col_sum(gy0 * r_.z0[l])))
        at = put(r_.gs_early, l, 512, dot_tn(r_.mb[l], dub))
        put(r_.gs_early, l, at, dot_tn(r_.g[l], db))
        r_.vT[...] = r_.vv[l].T
        r_.xeT[...] = r_.xe[l].T
        for hf in range(2):
            r_.qmT[hf] = r_.qm[l, hf].T

    def back_norms(l, k):
        s1, g1, s0, g0 = sync_finish(k, combine_sum)
        r_.gshift[l, 1:2] = s1
        r_.ggain[l, 1:2] = g1
        r_.gshift[l, 0:1] = s0
        r_.ggain[l, 0:1] = g0
        dmix = r_.dmix[...]
        d2 = r_.gain[l, 1:2] * r_.iv[l, 1:2] * (dmix - s1 / total - r_.z1[l] * (g1 / total))
        dab = d2.astype(BF16)
        r_.dxo[...] = dmix + d2
        r_.dob[...] = dot_nt(dab, r_.wo[l]).astype(BF16).astype(F32)
        put(r_.gs_early, l, 0, dot_tn(r_.ob[l], dab))
        r_.gkv[...] = jnp.zeros((2 * D, D), F32)
        r_.dq[...] = jnp.zeros((R, D), F32)

    def back_attention_block(l, i, between):
        t1 = (i + 1) % NB
        half = (zh + t1) % NB
        rows = pl.ds(pl.multiple_of(half * W, 128), W)

        def heads(hf, carry):
            lanes = lane_half(hf)
            dos = r_.dob[:, lanes] * r_.rb[l, (NB - t1) % NB, :, lanes]
            prod = dos * r_.oraw[l, :, lanes]
            for k in range(HK):
                r_.dom[k * R : (k + 1) * R] = jnp.where(lane_head == k, dos, 0.0).astype(BF16)
            parts = []
            for c in range(HK // 2):
                both = slice(2 * c * R, 2 * (c + 1) * R)
                dp = dot(r_.dom[both], r_.vT[lanes, rows])
                for k in range(2):
                    h = 2 * c + k
                    delta = jnp.sum(jnp.where(lane_head == h, prod, 0.0), 1, keepdims=True)
                    ds = r_.pst[l, head_rows(hf, h), rows].astype(F32) * (dp[k * R : (k + 1) * R] - delta)
                    r_.dss[h * R : (h + 1) * R] = ds.astype(BF16)
                part = dot(r_.dss[both], r_.kk[l, rows, lanes])
                parts += [part[0:R], part[R : 2 * R]]
            r_.dq[:, lanes] += by_head(parts)
            dk = dot(r_.qmT[hf], r_.dss[...]) * scale
            r_.dkv[pl.ds(pl.multiple_of(hf * 128, 128), 128)] = dk.astype(BF16)
            dv = dot(r_.dom[...].T, r_.pst[l, head_rows(hf, 0, HK), rows])
            r_.dkv[pl.ds(pl.multiple_of(D + hf * 128, 128), 128)] = dv.astype(BF16)
            between(i, hf)
            return carry

        lax.fori_loop(0, 2, heads, 0)
        dx = dot(r_.wqkv[l, :, D:], r_.dkv[...]).T
        r_.dxs[l, pl.ds(2 * half, 2)] = dx.astype(BF16).reshape(2, 2, R, D)

        @pl.when(i < NB - 1)
        def _():
            for low in range(2):
                zb = 2 * half + low
                send(r_.dxs.at[l, zb, 1 - par], r_.rs1.at[l, zb],
                     r_.rsp_s.at[l, 2 * i + low], r_.rsp_r.at[l, 2 * i + low], nodes=partner)

        @pl.when(i == NB - 1)
        def _():
            near = z_to(1)
            send(r_.dxs.at[l, z, 1 - par], r_.ro.at[l, 0], r_.ro_s.at[l, 0], r_.ro_r.at[l, 0], nodes=partner)
            send(r_.dxs.at[l, near, par], r_.ro.at[l, 1], r_.ro_s.at[l, 1], r_.ro_r.at[l, 1], nodes=2 * near + par)
            send(r_.dxs.at[l, near, 1 - par], r_.ro.at[l, 2], r_.ro_s.at[l, 2], r_.ro_r.at[l, 2],
                 nodes=2 * near + 1 - par)

        r_.gkv[...] += dot(r_.dkv[...], r_.xs[l, pl.ds(4 * half, 4)].reshape(W, D))

    def pass_on(l, i, t):
        zb = z_to(t)
        arrive(r_.rs1.at[l, zb], r_.rsp_r.at[l, 2 * i + zb % 2])
        both = r_.dxs[l, zb, par].astype(F32) + r_.rs1[l, zb].astype(F32)
        r_.cs[l, zb] = both.astype(BF16)
        send(r_.cs.at[l, zb], r_.rs2.at[l, z], r_.rsc_s.at[l, t], r_.rsc_r.at[l, t], nodes=2 * zb + par)

    def back_convolution(l):
        s0, g0 = r_.gshift[l, 0:1], r_.ggain[l, 0:1]
        inv_den = 1.0 / (r_.den[l] + GATE_EPS)
        n0 = r_.z0[l] * r_.gain[l, 0:1] + r_.shift[l, 0:1]
        gy0 = r_.dmix[...] * silu_slope(n0)
        dm = r_.gain[l, 0:1] * r_.iv[l, 0:1] * (gy0 - s0 / total - r_.z0[l] * (g0 / total))
        dnum = dm * inv_den
        dden = -dnum * r_.num[l] * inv_den
        dnum_e = select_rows(r_.T[...], dnum)
        dden_e = select_rows(r_.T[...], dden)
        gate = r_.gate[l]
        dgp = (dnum_e * r_.bs[l].astype(F32) + dden_e) * gate * (1.0 - gate)
        r_.dce[...] = dgp.astype(BF16)
        dpb = select_rows(r_.ST[...], dnum_e * gate).astype(BF16)
        dpe = select_rows(r_.ST[...], dgp).astype(BF16)
        dpd = select_rows(r_.TT[...], dgp).astype(BF16)
        dmb = dm.astype(BF16)
        dxe = dot_nt(dpb, r_.wp[l, :, D : 2 * D]) + dot_nt(dpe, r_.wp[l, :, 3 * D :])
        r_.hs[l, 0] = dxe[R : R + 32].astype(BF16)
        r_.hs[l, 1] = dxe[R + 32 : R + 64].astype(BF16)
        send(r_.hs.at[l, 0], r_.hr.at[l, 1], r_.hal_s.at[l, 0], r_.hal_r.at[l, 0], nodes=prev)
        send(r_.hs.at[l, 1], r_.hr.at[l, 0], r_.hal_s.at[l, 1], r_.hal_r.at[l, 1], nodes=nxt)
        r_.dxo[...] += (
            dxe[0:R]
            + dot_nt(dmb, r_.wp[l, :, 0:D])
            + dot_nt(dpd, r_.wp[l, :, 2 * D : 3 * D])
        )
        r_.dproj[0, 0:R] = dmb
        r_.dproj[1] = dpb
        r_.dproj[2, 0:R] = dpd
        r_.dproj[3] = dpe

    def conv_weight_grads(l):
        at = 0
        for c in range(4):
            width = R if c % 2 == 0 else 256
            at = put(r_.gs_conv, l, at, dot(r_.xeT[:, 0:width], r_.dproj[c, 0:width]))
        put(r_.gs_conv, l, at, dot(r_.efT[...], r_.dce[...]))

    def back_input(l):
        dx = r_.dxo[...]
        dx = dx + r_.dxs[l, z, par].astype(F32)
        for slot in range(3):
            arrive(r_.ro.at[l, slot], r_.ro_r.at[l, slot])
            dx = dx + r_.ro[l, slot].astype(F32)
        for t in range(2, NZ):
            c = z_from(t)
            arrive(r_.rs2.at[l, c], r_.rsc_r.at[l, t])
            dx = dx + r_.rs2[l, c].astype(F32)
        arrive(r_.hr.at[l, 0], r_.hal_r.at[l, 1])
        arrive(r_.hr.at[l, 1], r_.hal_r.at[l, 0])
        back = jnp.concatenate(
            [r_.hr[l, 0].astype(F32)[0:24], r_.hr[l, 1].astype(F32)[0:24], jnp.zeros((16, D), F32)], 0
        )
        return dx + dot(r_.A[...], back.astype(BF16))

    r_.dy[...] = r_.cot[...].astype(F32)

    E1, C1, Q1, E0, C0, QK0, V0 = range(len(GROUPS))

    def steps(*pairs):
        return [functools.partial(reduce_step, g, k) for g, k in pairs]

    def backward(b, carry):
        l = L - 1 - b
        first, last = b == 0, b == L - 1
        k = 4 + 2 * b
        back_feed_forward(l, k)
        when(last, *steps((E1, 8), (C1, 2), (Q1, 2)))
        back_norms(l, k)
        when(first, *steps((E1, 0)))
        when(last, *steps((C1, 3), (Q1, 3), (E0, 0)), functools.partial(back_convolution, l),
             functools.partial(conv_weight_grads, l), *steps((E0, 1), (C1, 4), (Q1, 4), (C0, 0)))

        def between(i, hf):
            when(first & (i == 0) & (hf == 0), *steps((E1, 1)))
            when(first & (i == 1) & (hf == 0), *steps((E1, 3)))
            when(first & (i == 1) & (hf == 1), *steps((E1, 4)))
            when(last & (i == 0) & (hf == 0), *steps((C0, 1)))
            when(last & (i == 0) & (hf == 1), *steps((C1, 5), (Q1, 5), (E0, 2)))
            when(last & (i == 1) & (hf == 0), *steps((C1, 6), (Q1, 6), (C0, 2), (E0, 3)))
            when(last & (i == 1) & (hf == 1), *steps((E0, 4), (C0, 3)))
            for t in range(2, NZ):
                when((i == 1) & (hf == 0), functools.partial(pass_on, l, 0, t))

        def block(i, carry):
            back_attention_block(l, i, between)
            when(first & (i == 0), functools.partial(back_convolution, l), *steps((E1, 2)))
            return carry

        lax.fori_loop(0, NB, block, 0)
        dqb = (r_.dq[...] * scale).astype(BF16)
        r_.dxo[...] += dot_nt(dqb, r_.wqkv[l, :, 0:D])
        when(first, functools.partial(conv_weight_grads, l), *steps((E1, 5), (C1, 0)))
        at = put(r_.gs_qkv, l, 0, dot(r_.xeT[:, 0:R], dqb))
        put(r_.gs_qkv, l, at, r_.gkv[...].T)
        when(last, *steps((QK0, 0), (V0, 0), (E0, 5), (C0, 4)))
        dx = back_input(l)
        r_.dy[...] = dx

        @pl.when(first)
        def _():
            below = L - 2
            zero_row = jnp.zeros((1, D), F32)
            sync_start(5, pack(col_sum(dx), col_sum(dx * r_.z2[below]), zero_row, zero_row))
            for step in steps((E1, 6), (Q1, 0)):
                step()
            s2, g2, _, _ = sync_finish(5, combine_sum)
            for step in steps((C1, 1), (Q1, 1), (E1, 7)):
                step()
            r_.gshift[below, 2:3] = s2
            r_.ggain[below, 2:3] = g2

        return carry

    lax.fori_loop(0, L, backward, 0)
    in_copy = pltpu.make_async_copy(r_.dy, r_.grad_in, r_.store.at[1])
    in_copy.start()
    for step in steps(
        (V0, 1), (QK0, 1), (C1, 7), (Q1, 7), (E0, 6), (C0, 5),
        (V0, 2), (QK0, 2), (C1, 8), (Q1, 8), (E0, 7), (C0, 6),
        (V0, 3), (QK0, 3), (E0, 8), (C0, 7),
        (V0, 4), (QK0, 4), (C0, 8),
    ):
        step()
    for l in range(L):
        for k in range(3):
            r_.ggain_out[k, l : l + 1] = r_.ggain[l, k : k + 1]
            r_.gshift_out[k, l : l + 1] = r_.gshift[l, k : k + 1]
    for g in range(len(GROUPS)):
        reduce_drain(g)
    sent(r_.meta.at[0 : N - 1], r_.meta_s.at[0])
    for k in range(SYNCS):
        sent(r_.st1.at[k, 0 : M * N - 1], r_.st1_s.at[k])
    for l in range(L):
        for t in range(NZ):
            sent(r_.gb.at[l, 0], r_.agp_s.at[l, t])
            if t > 0:
                sent(r_.gb.at[l, 0], r_.agc_s.at[l, t])
            if t > 1:
                sent(r_.rs1.at[l, 0], r_.rsc_s.at[l, t])
        for slot in range(2 * (NB - 1)):
            sent(r_.rs1.at[l, 0], r_.rsp_s.at[l, slot])
        for slot in range(3):
            sent(r_.ro.at[l, 0], r_.ro_s.at[l, slot])
        for side in range(2):
            sent(r_.hs.at[l, 0], r_.hal_s.at[l, side])
    act_copy.wait()
    in_copy.wait()


def finish_kernel(act_h, gin_h, *refs):
    n = len(GROUPS)
    held, (ggain_h, gshift_h), refs = refs[:n], refs[n : n + 2], refs[n + 2 :]
    act_o, gin_o, proj_o, edge_o, qkv_o, out_o, up_o, down_o, ggain_o, gshift_o = refs[:10]
    summed, refs = refs[10 : 10 + n], refs[10 + n :]
    act, gin, proj, edge, qkv, out, up, down, in_sem, out_sem = refs
    loads = [
        pltpu.make_async_copy(src, dst, in_sem.at[i])
        for i, (src, dst) in enumerate(zip(held + (act_h, gin_h), summed + (act, gin), strict=True))
    ]
    for load in loads:
        load.start()
    ggain_o[...] = ggain_h[...]
    gshift_o[...] = gshift_h[...]
    stores = []

    def store(src, dst):
        copy = pltpu.make_async_copy(src, dst, out_sem.at[len(stores)])
        copy.start()
        stores.append(copy)

    def widen(dst, l, g, at, first=0, last=None):
        rows = dst.shape[1]
        for c in range(first, dst.shape[2] // 128 if last is None else last):
            dst[l, :, 128 * c : 128 * (c + 1)] = summed[g][at : at + rows].astype(F32)
            at += rows
        return at

    for g, (name, l, first, rows, _) in enumerate(GROUPS):
        loads[g].wait()
        if name == "early":
            at = widen(out, l, g, 0)
            store(out.at[l], out_o.at[l])
            at = widen(up, l, g, at)
            store(up.at[l], up_o.at[l])
            widen(down, l, g, at)
            store(down.at[l], down_o.at[l])
        elif name == "conv":
            at = widen(proj, l, g, 0)
            store(proj.at[l], proj_o.at[l])
            widen(edge, l, g, at)
            store(edge.at[l], edge_o.at[l])
        else:
            widen(qkv, l, g, 0, first // 256, (first + rows) // 256)
            if first + rows == 1536:
                store(qkv.at[l], qkv_o.at[l])
    for i, (src, dst) in enumerate(((act, act_o), (gin, gin_o))):
        loads[n + i].wait()
        store(src, dst)
    for copy in stores:
        copy.wait()


def fused_device(
    N, M, node_input, edge_feat, graph_ids, edge_src, edge_dst, halo_send, w_proj, w_edge, w_qkv,
    w_out, w_up, w_down, norm_gain, norm_shift, cotangent,
):
    R, D = node_input.shape
    E = edge_feat.shape[0]
    L = w_proj.shape[0]
    names = scratch_list(N, M, L, R, E)
    vmem = pl.BlockSpec(memory_space=pltpu.VMEM)
    hbm = pl.BlockSpec(memory_space=pltpu.HBM)
    shape = jax.ShapeDtypeStruct
    rows = shape((R, D), F32)
    norm = shape((3, L, D), F32)
    groups = [shape((rows_g, 128), BF16) for _, _, _, rows_g, _ in GROUPS]
    outs = pl.pallas_call(
        functools.partial(kernel, N, M, L, tuple(names)),
        out_shape=[rows, rows, *groups, norm, norm],
        in_specs=[hbm] + [vmem] * 4 + [hbm] * 7 + [vmem] * 2 + [hbm],
        out_specs=[hbm] * (2 + len(GROUPS)) + [vmem] * 2,
        scratch_shapes=list(names.values()),
        compiler_params=pltpu.CompilerParams(
            collective_id=0, has_side_effects=True, vmem_limit_bytes=60 << 20
        ),
        name="layers",
    )(node_input, graph_ids, edge_src, edge_dst, halo_send, edge_feat, w_proj, w_edge, w_qkv, w_out, w_up,
      w_down, norm_gain.transpose(1, 0, 2), norm_shift.transpose(1, 0, 2), cotangent)
    weights = [shape(w.shape, F32) for w in (w_proj, w_edge, w_qkv, w_out, w_up, w_down)]
    results = pl.pallas_call(
        finish_kernel,
        out_shape=[rows, rows, *weights, norm, norm],
        in_specs=[hbm] * (2 + len(GROUPS)) + [vmem] * 2,
        out_specs=[hbm] * 8 + [vmem] * 2,
        scratch_shapes=[pltpu.VMEM(s.shape, s.dtype) for s in (*groups, rows, rows, *weights)]
        + [pltpu.SemaphoreType.DMA((len(GROUPS) + 2,)), pltpu.SemaphoreType.DMA((14,))],
        compiler_params=pltpu.CompilerParams(vmem_limit_bytes=60 << 20),
        name="gradients",
    )(*outs)
    ggain, gshift = results[8].transpose(1, 0, 2), results[9].transpose(1, 0, 2)
    return (*results[:8], ggain, gshift)


BLOCK_CAP = 2048


def extended_2(block, sides, width):
    for axis, dim in sides:
        count = lax.axis_size(axis)
        forward = [(i, i + 1) for i in range(count - 1)]
        forward.append((count - 1, 0))
        backward = [(target, source) for source, target in forward]
        low = lax.ppermute(
            lax.slice_in_dim(block, block.shape[dim] - width, None, axis=dim), axis, forward
        )
        high = lax.ppermute(lax.slice_in_dim(block, 0, width, axis=dim), axis, backward)
        block = jnp.concatenate([low, block, high], axis=dim)
    return block


def block_length(total_rows, upper_limit):
    for length in range(min(total_rows, upper_limit), 0, -1):
        if total_rows % length == 0:
            return length
    return 1


def outer_product(left, right):
    return lax.dot_general(
        left, right, (((0,), (0,)), ((), ())), preferred_element_type=jnp.float32
    )


def times_transposed(left, weight):
    return lax.dot_general(
        left, weight, (((1,), (1,)), ((), ())), preferred_element_type=jnp.float32
    )


def forward_product(left, weight):
    return jnp.dot(left, weight, preferred_element_type=jnp.float32)


def silu_slope_plain(inputs):
    logistic = jax.nn.sigmoid(inputs)
    return logistic * (1.0 + inputs * (1.0 - logistic))


def normalize(inputs, gain_row, shift_row, node_total):
    batch_mean = lax.psum(jnp.sum(inputs, 0), ("nodes", "rep")) / node_total
    centred = inputs - batch_mean
    batch_var = lax.psum(jnp.sum(centred * centred, 0), ("nodes", "rep")) / node_total
    inv_std = lax.rsqrt(batch_var + NORM_EPS)
    standard = (inputs - batch_mean) * inv_std
    return (standard * gain_row + shift_row, standard, inv_std)


def normalize_back(grad_out, standard, inv_std, gain_row, node_total):
    shift_grad, gain_grad = lax.psum(
        (jnp.sum(grad_out, 0), jnp.sum(grad_out * standard, 0)), ("nodes", "rep")
    )
    grad_in = (
        gain_row
        * inv_std
        * (grad_out - shift_grad / node_total - standard * gain_grad / node_total)
    )
    return (grad_in, gain_grad, shift_grad)


def exchange_sources(outgoing):
    halo_rows = outgoing.shape[0] // 2
    grown = extended_2(outgoing, (("nodes", 0),), halo_rows)
    return jnp.concatenate([grown[:halo_rows], grown[3 * halo_rows :]], 0)


def return_sources(incoming_grad):
    halo_rows = incoming_grad.shape[0] // 2
    grown = extended_2(incoming_grad.astype(jnp.bfloat16), (("nodes", 0),), halo_rows).astype(
        incoming_grad.dtype
    )
    return jnp.concatenate([grown[:halo_rows], grown[3 * halo_rows :]], 0)


def attend_forward(query_rows, key_rows, value_rows, local_graphs, group_graphs):
    row_count = query_rows.shape[0]
    score_scale = HEAD_DIM ** (-0.5)
    queries = query_rows.reshape(row_count, HEADS, HEAD_DIM)

    def add_piece(carried, kv_piece, first_row):
        key_piece, value_piece = kv_piece
        piece_rows = key_piece.shape[0]
        block_len = block_length(piece_rows, BLOCK_CAP)

        def add_block(block_state, block_index):
            row_max, row_sum, accumulated = block_state
            block_start = block_index * block_len
            key_block = lax.dynamic_slice_in_dim(key_piece, block_start, block_len, 0).reshape(
                block_len, HEADS, HEAD_DIM
            )
            value_block = lax.dynamic_slice_in_dim(value_piece, block_start, block_len, 0).reshape(
                block_len, HEADS, HEAD_DIM
            )
            key_graphs = lax.dynamic_slice_in_dim(
                group_graphs, first_row + block_start, block_len, 0
            )
            same_graph = (local_graphs[:, None] == key_graphs[None, :])[None]
            scores = (
                jnp.einsum("qhd,khd->hqk", queries, key_block, preferred_element_type=jnp.float32)
                * score_scale
            )
            scores = jnp.where(same_graph, scores, NEG)
            new_max = jnp.maximum(row_max, jnp.max(scores, 2))
            weights = jnp.where(same_graph, jnp.exp(scores - new_max[:, :, None]), 0.0)
            factor = jnp.exp(row_max - new_max)
            row_sum = row_sum * factor + jnp.sum(weights, 2)
            contrib = jnp.einsum(
                "hqk,khd->qhd",
                weights.astype(jnp.bfloat16),
                value_block,
                preferred_element_type=jnp.float32,
            )
            accumulated = accumulated * jnp.transpose(factor)[:, :, None] + contrib
            return ((new_max, row_sum, accumulated), None)

        carried, _ = lax.scan(add_block, carried, jnp.arange(piece_rows // block_len))
        return carried

    start_state = (
        jnp.full((HEADS, row_count), NEG, jnp.float32),
        jnp.zeros((HEADS, row_count), jnp.float32),
        jnp.zeros((row_count, HEADS, HEAD_DIM), jnp.float32),
    )
    row_max, row_sum, accumulated = add_piece(
        start_state,
        (
            lax.all_gather(key_rows, "nodes", axis=0, tiled=True),
            lax.all_gather(value_rows, "nodes", axis=0, tiled=True),
        ),
        jnp.int32(0),
    )
    attn_raw = accumulated / jnp.transpose(row_sum)[:, :, None]
    log_sum = row_max + jnp.log(row_sum)
    return (attn_raw, log_sum)


def attend_backward(
    query_rows, key_rows, value_rows, grad_low, attn_raw, log_sum, local_graphs, group_graphs
):
    row_count = query_rows.shape[0]
    model_width = HEADS * HEAD_DIM
    score_scale = HEAD_DIM ** (-0.5)
    queries = query_rows.reshape(row_count, HEADS, HEAD_DIM)
    grad_heads = grad_low.reshape(row_count, HEADS, HEAD_DIM)
    row_delta = jnp.einsum("qhd,qhd->hq", grad_heads.astype(jnp.float32), attn_raw)

    def score_block(key_block, value_block, key_graphs):
        same_graph = (local_graphs[:, None] == key_graphs[None, :])[None]
        scores = (
            jnp.einsum("qhd,khd->hqk", queries, key_block, preferred_element_type=jnp.float32)
            * score_scale
        )
        attn_weights = jnp.exp(jnp.where(same_graph, scores - log_sum[:, :, None], NEG))
        grad_weights = jnp.einsum(
            "qhd,khd->hqk", grad_heads, value_block, preferred_element_type=jnp.float32
        )
        grad_scores = (attn_weights * (grad_weights - row_delta[:, :, None])).astype(jnp.bfloat16)
        return (attn_weights, grad_scores)

    def key_terms(attn_weights, grad_scores, block_len):
        grad_keys = (
            jnp.einsum("hqk,qhd->khd", grad_scores, queries, preferred_element_type=jnp.float32)
            * score_scale
        )
        grad_values = jnp.einsum(
            "hqk,qhd->khd",
            attn_weights.astype(jnp.bfloat16),
            grad_heads,
            preferred_element_type=jnp.float32,
        )
        return jnp.concatenate(
            [
                grad_keys.reshape(block_len, model_width),
                grad_values.reshape(block_len, model_width),
            ],
            1,
        )

    def query_term(grad_scores, key_block):
        return (
            jnp.einsum("hqk,khd->qhd", grad_scores, key_block, preferred_element_type=jnp.float32)
            * score_scale
        )

    group_rows = group_graphs.shape[0]

    def add_piece(carried, kv_piece, first_row):
        key_piece, value_piece = kv_piece
        piece_rows = key_piece.shape[0]
        block_len = block_length(piece_rows, BLOCK_CAP)

        def add_block(block_state, block_index):
            grad_query, buffer = block_state
            block_start = block_index * block_len
            key_block = lax.dynamic_slice_in_dim(key_piece, block_start, block_len, 0).reshape(
                block_len, HEADS, HEAD_DIM
            )
            value_block = lax.dynamic_slice_in_dim(value_piece, block_start, block_len, 0).reshape(
                block_len, HEADS, HEAD_DIM
            )
            place = first_row + block_start
            key_graphs = lax.dynamic_slice_in_dim(group_graphs, place, block_len, 0)
            attn_weights, grad_scores = score_block(key_block, value_block, key_graphs)
            grad_query = grad_query + query_term(grad_scores, key_block)
            block_terms = key_terms(attn_weights, grad_scores, block_len)
            current = lax.dynamic_slice_in_dim(buffer, place, block_len, 0)
            buffer = lax.dynamic_update_slice_in_dim(buffer, current + block_terms, place, 0)
            return ((grad_query, buffer), None)

        carried, _ = lax.scan(add_block, carried, jnp.arange(piece_rows // block_len))
        return carried

    start_state = (
        jnp.zeros((row_count, HEADS, HEAD_DIM), jnp.float32),
        jnp.zeros((group_rows, 2 * model_width), jnp.float32),
    )
    grad_query, buffer = add_piece(
        start_state,
        (
            lax.all_gather(key_rows, "nodes", axis=0, tiled=True),
            lax.all_gather(value_rows, "nodes", axis=0, tiled=True),
        ),
        jnp.int32(0),
    )
    grad_kv = lax.psum_scatter(buffer, "nodes", scatter_dimension=0, tiled=True)
    return (
        grad_query.reshape(row_count, model_width),
        grad_kv[:, :model_width],
        grad_kv[:, model_width:],
    )


def layer_forward(
    hidden, params, edge_feat, edge_src, edge_dst, halo_send, local_graphs, group_graphs, node_total
):
    w_proj, w_edge, w_qkv, w_out, w_up, w_down, norm_gains, norm_shifts = params
    row_count, model_width = hidden.shape
    hidden_low = hidden.astype(jnp.bfloat16)
    projected = forward_product(hidden_low, w_proj)
    self_term = projected[:, :model_width]
    dest_term = projected[:, 2 * model_width : 3 * model_width]
    source_rows = jnp.concatenate(
        [projected[:, model_width : 2 * model_width], projected[:, 3 * model_width :]], 1
    ).astype(jnp.bfloat16)
    incoming = exchange_sources(source_rows[halo_send])
    extended = jnp.concatenate([source_rows, incoming], 0)
    edge_rows = extended[edge_src].astype(jnp.float32)
    source_b = edge_rows[:, :model_width]
    source_e = edge_rows[:, model_width:]
    edge_proj = forward_product(edge_feat, w_edge)
    gating = jax.nn.sigmoid(dest_term[edge_dst] + source_e + edge_proj)
    numerator = jax.ops.segment_sum(gating * source_b, edge_dst, row_count)
    denominator = jax.ops.segment_sum(gating, edge_dst, row_count)
    message = self_term + numerator / (denominator + GATE_EPS)
    normed_one, standard_one, inv_one = normalize(
        message, norm_gains[0], norm_shifts[0], node_total
    )
    local_out = hidden + jax.nn.silu(normed_one)
    qkv_low = forward_product(hidden_low, w_qkv).astype(jnp.bfloat16)
    query_rows = qkv_low[:, :model_width]
    key_rows = qkv_low[:, model_width : 2 * model_width]
    value_rows = qkv_low[:, 2 * model_width :]
    attn_raw, log_sum = attend_forward(query_rows, key_rows, value_rows, local_graphs, group_graphs)
    attn_low = attn_raw.reshape(row_count, model_width).astype(jnp.bfloat16)
    attn_proj = forward_product(attn_low, w_out)
    normed_two, standard_two, inv_two = normalize(
        hidden + attn_proj, norm_gains[1], norm_shifts[1], node_total
    )
    mixed = local_out + normed_two
    mixed_low = mixed.astype(jnp.bfloat16)
    up_proj = forward_product(mixed_low, w_up)
    activated = jax.nn.silu(up_proj).astype(jnp.bfloat16)
    down_proj = forward_product(activated, w_down)
    normed_three, standard_three, inv_three = normalize(
        mixed + down_proj, norm_gains[2], norm_shifts[2], node_total
    )
    saved = (
        hidden_low,
        source_b,
        gating,
        numerator,
        denominator,
        normed_one,
        standard_one,
        inv_one,
        query_rows,
        key_rows,
        value_rows,
        attn_raw,
        log_sum,
        attn_low,
        standard_two,
        inv_two,
        mixed_low,
        up_proj,
        activated,
        standard_three,
        inv_three,
    )
    return (normed_three, saved)


def layer_backward(
    grad_out,
    params,
    saved,
    edge_feat,
    edge_src,
    edge_dst,
    halo_send,
    local_graphs,
    group_graphs,
    node_total,
):
    w_proj, w_edge, w_qkv, w_out, w_up, w_down, norm_gains, norm_shifts = params
    (
        hidden_low,
        source_b,
        gating,
        numerator,
        denominator,
        normed_one,
        standard_one,
        inv_one,
        query_rows,
        key_rows,
        value_rows,
        attn_raw,
        log_sum,
        attn_low,
        standard_two,
        inv_two,
        mixed_low,
        up_proj,
        activated,
        standard_three,
        inv_three,
    ) = saved
    row_count, model_width = grad_out.shape
    grad_three, gain_three, shift_three = normalize_back(
        grad_out, standard_three, inv_three, norm_gains[2], node_total
    )
    down_grad = grad_three.astype(jnp.bfloat16)
    grad_w_down = outer_product(activated, down_grad)
    up_grad = (times_transposed(down_grad, w_down) * silu_slope_plain(up_proj)).astype(jnp.bfloat16)
    grad_w_up = outer_product(mixed_low, up_grad)
    grad_mixed = grad_three + times_transposed(up_grad, w_up)
    grad_two, gain_two, shift_two = normalize_back(
        grad_mixed, standard_two, inv_two, norm_gains[1], node_total
    )
    out_grad = grad_two.astype(jnp.bfloat16)
    grad_w_out = outer_product(attn_low, out_grad)
    attn_grad = times_transposed(out_grad, w_out).astype(jnp.bfloat16)
    grad_query, grad_key, grad_value = attend_backward(
        query_rows, key_rows, value_rows, attn_grad, attn_raw, log_sum, local_graphs, group_graphs
    )
    qkv_grad = jnp.concatenate([grad_query, grad_key, grad_value], 1).astype(jnp.bfloat16)
    grad_w_qkv = outer_product(hidden_low, qkv_grad)
    grad_message, gain_one, shift_one = normalize_back(
        grad_mixed * silu_slope_plain(normed_one), standard_one, inv_one, norm_gains[0], node_total
    )
    shifted = denominator + GATE_EPS
    grad_numer = grad_message / shifted
    grad_denom = -grad_message * numerator / (shifted * shifted)
    numer_edge = grad_numer[edge_dst]
    grad_gate = numer_edge * source_b + grad_denom[edge_dst]
    grad_pre_edge = grad_gate * gating * (1.0 - gating)
    edge_grad = grad_pre_edge.astype(jnp.bfloat16)
    grad_w_edge = outer_product(edge_feat, edge_grad)
    grad_dest = jax.ops.segment_sum(grad_pre_edge, edge_dst, row_count)
    grad_extended = jax.ops.segment_sum(
        jnp.concatenate([numer_edge * gating, grad_pre_edge], 1),
        edge_src,
        row_count + halo_send.shape[0],
    )
    returned = return_sources(grad_extended[row_count:])
    grad_source = grad_extended[:row_count].at[halo_send].add(returned)
    proj_grad = jnp.concatenate(
        [grad_message, grad_source[:, :model_width], grad_dest, grad_source[:, model_width:]], 1
    ).astype(jnp.bfloat16)
    grad_w_proj = outer_product(hidden_low, proj_grad)
    grad_hidden = (
        grad_mixed
        + grad_two
        + times_transposed(proj_grad, w_proj)
        + times_transposed(qkv_grad, w_qkv)
    )
    weight_grads = (grad_w_proj, grad_w_edge, grad_w_qkv, grad_w_out, grad_w_up, grad_w_down)
    return (
        grad_hidden,
        weight_grads,
        jnp.stack([gain_one, gain_two, gain_three]),
        jnp.stack([shift_one, shift_two, shift_three]),
    )


def per_device(
    node_input,
    edge_feat,
    graph_ids,
    edge_src,
    edge_dst,
    halo_send,
    w_proj,
    w_edge,
    w_qkv,
    w_out,
    w_up,
    w_down,
    norm_gain,
    norm_shift,
    cotangent,
):
    group_graphs = lax.all_gather(graph_ids, "nodes", axis=0, tiled=True)
    node_total = node_input.shape[0] * lax.axis_size("nodes") * lax.axis_size("rep")
    layer_count = w_proj.shape[0]
    layer_params = [
        (
            w_proj[layer_index],
            w_edge[layer_index],
            w_qkv[layer_index],
            w_out[layer_index],
            w_up[layer_index],
            w_down[layer_index],
            norm_gain[layer_index],
            norm_shift[layer_index],
        )
        for layer_index in range(layer_count)
    ]
    hidden = node_input.astype(jnp.float32)
    saved_all = []
    for layer_index in range(layer_count):
        hidden, saved = layer_forward(
            hidden,
            layer_params[layer_index],
            edge_feat,
            edge_src,
            edge_dst,
            halo_send,
            graph_ids,
            group_graphs,
            node_total,
        )
        saved_all.append(saved)
    grad_hidden = cotangent.astype(jnp.float32)
    weight_parts = [None] * layer_count
    gain_parts = [None] * layer_count
    shift_parts = [None] * layer_count
    for layer_index in range(layer_count - 1, -1, -1):
        (
            grad_hidden,
            weight_parts[layer_index],
            gain_parts[layer_index],
            shift_parts[layer_index],
        ) = layer_backward(
            grad_hidden,
            layer_params[layer_index],
            saved_all[layer_index],
            edge_feat,
            edge_src,
            edge_dst,
            halo_send,
            graph_ids,
            group_graphs,
            node_total,
        )
    proj_local = jnp.stack([weight_parts[layer_index][0] for layer_index in range(layer_count)])
    edge_local = jnp.stack([weight_parts[layer_index][1] for layer_index in range(layer_count)])
    qkv_local = jnp.stack([weight_parts[layer_index][2] for layer_index in range(layer_count)])
    out_local = jnp.stack([weight_parts[layer_index][3] for layer_index in range(layer_count)])
    up_local = jnp.stack([weight_parts[layer_index][4] for layer_index in range(layer_count)])
    down_local = jnp.stack([weight_parts[layer_index][5] for layer_index in range(layer_count)])
    grad_proj, grad_edge, grad_qkv, grad_out, grad_up, grad_down = lax.psum(
        (proj_local, edge_local, qkv_local, out_local, up_local, down_local), ("nodes", "rep")
    )
    return (
        hidden,
        grad_hidden,
        grad_proj,
        grad_edge,
        grad_qkv,
        grad_out,
        grad_up,
        grad_down,
        jnp.stack(gain_parts),
        jnp.stack(shift_parts),
    )


def solution(mesh):
    in_specs = (
        P(("rep", "nodes"), None),
        P(("rep", "nodes"), None),
        P(("rep", "nodes")),
        P(("rep", "nodes")),
        P(("rep", "nodes")),
        P(("rep", "nodes")),
        P(),
        P(),
        P(),
        P(),
        P(),
        P(),
        P(),
        P(),
        P(("rep", "nodes"), None),
    )
    out_specs = (
        P(("rep", "nodes"), None),
        P(("rep", "nodes"), None),
        P(),
        P(),
        P(),
        P(),
        P(),
        P(),
        P(),
        P(),
    )
    N, M = mesh.shape["nodes"], mesh.shape["rep"]
    fused = N in (4, 8) and M % 2 == 0 and 512 % (16 * N * M) == 0
    return jax.shard_map(
        functools.partial(fused_device, N, M) if fused else per_device,
        mesh=mesh, in_specs=in_specs, out_specs=out_specs, check_vma=False,
    )
```

```python
import functools
import math

import jax
import jax.numpy as jnp
from jax import lax
from jax.experimental import pallas as pl
from jax.experimental.pallas import tpu as pltpu
from jax.sharding import PartitionSpec as P

HEADS = 8
HEAD_DIM = 32
NEG = -1e30
NORM_EPS = 1e-05
GATE_EPS = 1e-06
F32, BF16, I32 = jnp.float32, jnp.bfloat16, jnp.int32
MESH = pl.DeviceIdType.MESH
SYNCS = 7
GROUPS = (
    ("early", 1, 0, 2560, ("core", "y", "nodes")),
    ("conv", 1, 0, 2560, ("core", "y", "nodes")),
    ("qkv", 1, 0, 1536, ("core", "y", "nodes")),
    ("early", 0, 0, 2560, ("core", "y", "nodes")),
    ("conv", 0, 0, 2560, ("core", "y", "nodes")),
    ("qkv", 0, 0, 1024, ("rep", "nodes")),
    ("qkv", 0, 1024, 512, ("nodes", "rep")),
)


def dot(left, right):
    return lax.dot_general(
        left, right, (((1,), (0,)), ((), ())), preferred_element_type=F32
    )


def dot_nt(left, right):
    return lax.dot_general(
        left, right, (((1,), (1,)), ((), ())), preferred_element_type=F32
    )


def dot_tn(left, right):
    return lax.dot_general(
        left, right, (((0,), (0,)), ((), ())), preferred_element_type=F32
    )


def split(value):
    high = value.astype(BF16)
    return high, (value - high.astype(F32)).astype(BF16)


def select_rows(onehot, value):
    high, low = split(value)
    return dot(onehot, high) + dot(onehot, low)


def sigmoid(value):
    return 1.0 / (1.0 + jnp.exp(-value))


def silu_slope(value):
    logistic = sigmoid(value)
    return logistic * (1.0 + value * (1.0 - logistic))


def col_sum(value):
    return jnp.sum(value, axis=0, keepdims=True)


def pack(first, second, third, fourth):
    halves = []
    for row in (first, second, third, fourth):
        halves += [row[:, :128], row[:, 128:]]
    return jnp.concatenate(halves, 0)


def unpack(tile):
    return [
        jnp.concatenate([tile[2 * i : 2 * i + 1], tile[2 * i + 1 : 2 * i + 2]], 1)
        for i in range(4)
    ]


def combine_pair(tiles, count):
    mean = jnp.mean(tiles[:, 0:4], 0)
    off = tiles[:, 0:4] - mean
    return jnp.concatenate([mean, jnp.sum(tiles[:, 4:8] + count * off * off, 0)], 0)


def combine_last(tiles, count):
    mean = jnp.mean(tiles[:, 0:2], 0)
    off = tiles[:, 0:2] - mean
    return jnp.concatenate(
        [
            mean,
            jnp.sum(tiles[:, 2:4], 0),
            jnp.sum(tiles[:, 4:6] + count * off * off, 0),
            jnp.sum(tiles[:, 6:8] + off * tiles[:, 2:4], 0),
        ],
        0,
    )


def combine_sum(tiles, count):
    return jnp.sum(tiles, 0)


class Refs:
    pass


def axis_sizes(N, M):
    return dict(core=2, y=M // 2, x=2, z=N // 2, rep=M, nodes=N)


def scratch_list(N, M, L, R, E):
    NZ, NB, G = N // 2, N // 4, N * R
    D, FF, W, HH = 256, 512, 4 * R, HEADS // 2 * R
    dma = lambda *shape: pltpu.SemaphoreType.DMA(shape)
    vm = lambda dtype, *shape: pltpu.VMEM(shape, dtype)
    names = dict(
        gb=vm(BF16, L, N, R, D),
        xs=vm(BF16, L, N, R, D),
        meta=vm(I32, N, 8, 256),
        ef=vm(BF16, E, D),
        cot=vm(BF16, R, D),
        wp=vm(BF16, L, D, 4 * D),
        we=vm(BF16, L, D, D),
        wqkv=vm(BF16, L, D, 3 * D),
        wo=vm(BF16, L, D, D),
        wu=vm(BF16, L, D, FF),
        wd=vm(BF16, L, FF, D),
        st1=vm(F32, SYNCS, M * N, 8, 128),
        gain=vm(F32, L, 8, D),
        shift=vm(F32, L, 8, D),
        ggain=vm(F32, L, 8, D),
        gshift=vm(F32, L, 8, D),
        iv=vm(F32, L, 8, D),
        moff=vm(F32, N, 8, D),
        move=vm(F32, 8, D),
        T=vm(BF16, E, R),
        TT=vm(BF16, R, E),
        S=vm(BF16, E, 256),
        ST=vm(BF16, 256, E),
        efT=vm(BF16, D, E),
        HP=vm(BF16, 32, R),
        HN=vm(BF16, 32, R),
        A=vm(BF16, R, 64),
        bias=vm(F32, R, G),
        ce=vm(F32, L, E, D),
        xf=vm(F32, L + 1, R, D),
        xe=vm(BF16, L, 256, D),
        xeT=vm(BF16, D, 256),
        gate=vm(F32, L, E, D),
        bs=vm(BF16, L, E, D),
        num=vm(F32, L, R, D),
        den=vm(F32, L, R, D),
        z0=vm(F32, L, R, D),
        z1=vm(F32, L, R, D),
        z2=vm(F32, L, R, D),
        kk=vm(BF16, L, G, D),
        vv=vm(BF16, L, G, D),
        kT=vm(BF16, D, G),
        vT=vm(BF16, D, G),
        od=vm(F32, NB, R, D),
        md=vm(F32, NB, R, D),
        ld=vm(F32, NB, R, D),
        rb=vm(F32, L, NB, R, D),
        pst=vm(BF16, L, HEADS * R, G),
        oraw=vm(F32, L, R, D),
        ob=vm(BF16, L, R, D),
        mb=vm(BF16, L, R, D),
        u=vm(F32, L, R, FF),
        g=vm(BF16, L, R, FF),
        dy=vm(F32, R, D),
        dmix=vm(F32, R, D),
        dxo=vm(F32, R, D),
        dob=vm(F32, R, D),
        dq=vm(F32, R, D),
        qm=vm(BF16, L, 2, HH, 128),
        qmT=vm(BF16, 2, 128, HH),
        dom=vm(BF16, HH, 128),
        dss=vm(BF16, HH, W),
        dkv=vm(BF16, 2 * D, W),
        gkv=vm(F32, 2 * D, D),
        dce=vm(BF16, E, D),
        dproj=vm(BF16, 4, 256, D),
        dxs=vm(BF16, L, NZ, 2, R, D),
        rs1=vm(BF16, L, NZ, R, D),
        cs=vm(BF16, L, NZ, R, D),
        rs2=vm(BF16, L, NZ, R, D),
        ro=vm(BF16, L, 3, R, D),
        hs=vm(BF16, L, 2, 32, D),
        hr=vm(BF16, L, 2, 32, D),
    )
    names.update(
        gs_early=vm(BF16, L, 2560, 128),
        gs_conv=vm(BF16, L, 2560, 128),
        gs_qkv=vm(BF16, L, 1536, 128),
    )
    sizes = axis_sizes(N, M)
    for g, (_, _, _, rows, stages) in enumerate(GROUPS):
        names[f"go{g}"] = vm(BF16, rows, 128)
        left = rows
        for k, axis in enumerate(stages):
            left //= sizes[axis]
            names[f"ga{g}_{k}"] = vm(BF16, sizes[axis] - 1, left, 128)
            if k < len(stages) - 1:
                names[f"gh{g}_{k}"] = vm(BF16, left, 128)
    names.update(
        ar_s=dma(len(GROUPS), 8),
        ar_r=dma(len(GROUPS), 8),
        ar_l=dma(len(GROUPS)),
        load=dma(10),
        store=dma(2),
        meta_s=dma(1),
        meta_r=dma(1),
        st1_s=dma(SYNCS),
        st1_r=dma(SYNCS),
        agc_s=dma(L, NZ),
        agc_r=dma(L, NZ),
        agp_s=dma(L, NZ),
        agp_r=dma(L, NZ),
        rsp_s=dma(L, NZ),
        rsp_r=dma(L, NZ),
        ro_s=dma(L, 3),
        ro_r=dma(L, 3),
        rsc_s=dma(L, NZ),
        rsc_r=dma(L, NZ),
        hal_s=dma(L, 2),
        hal_r=dma(L, 2),
    )
    return names


IN_NAMES = (
    "x_in", "ids", "edge_src", "edge_dst", "halo", "ef_h", "wp_h", "we_h", "wqkv_h", "wo_h", "wu_h", "wd_h",
    "gain_in", "shift_in", "cot_h",
)
OUT_NAMES = ("out_act", "grad_in", *(f"gout{g}" for g in range(len(GROUPS))), "ggain_out", "gshift_out")


def kernel(N, M, L, names, *args):
    r_ = Refs()
    for name, ref in zip(IN_NAMES + OUT_NAMES + tuple(names), args, strict=True):
        setattr(r_, name, ref)
    R, D = r_.x_in.shape
    E = r_.ef.shape[0]
    NZ, NB, G, W = N // 2, N // 4, N * R, 4 * R
    HK = HEADS // 2
    total = float(N * M * R)
    scale = HEAD_DIM ** -0.5
    me = lax.axis_index("nodes")
    rep = lax.axis_index("rep")
    z = me // 2
    par = me % 2
    partner = 2 * z + (1 - par)
    prev = (me + N - 1) % N
    nxt = (me + 1) % N
    zh, zl = z // 2, z % 2
    z_to = lambda t: 2 * ((zh + t // 2) % NB) + (zl + t % 2) % 2
    z_from = lambda t: 2 * ((zh + NB - t // 2) % NB) + (zl + t % 2) % 2

    def remote(src, dst, s_sem, r_sem, **where):
        return pltpu.make_async_remote_copy(
            src_ref=src, dst_ref=dst, send_sem=s_sem, recv_sem=r_sem,
            device_id=where, device_id_type=MESH,
        )

    def send(src, dst, s_sem, r_sem, **where):
        remote(src, dst, s_sem, r_sem, **where).start()

    def arrive(dst, r_sem):
        remote(dst, dst, r_sem, r_sem, nodes=partner).wait_recv()

    def sent(src, s_sem):
        remote(src, src, s_sem, s_sem, nodes=partner).wait_send()

    def when(condition, *acts):
        @pl.when(condition)
        def _():
            for act in acts:
                act()

    loads = [
        pltpu.make_async_copy(getattr(r_, f"{name}_h"), getattr(r_, name), r_.load.at[i])
        for i, name in enumerate(("ef", "we", "wqkv", "wp", "wo", "wu", "wd", "cot"))
    ]
    own_rows = pltpu.make_async_copy(r_.x_in, r_.gb.at[0, me], r_.load.at[8])
    own_rows.start()
    for load in loads:
        load.start()

    barrier = pltpu.get_barrier_semaphore()
    for dr in range(M):
        for d in range(N):
            if dr + d > 0:
                pl.semaphore_signal(barrier, inc=1, device_id={"rep": (rep + dr) % M, "nodes": (me + d) % N},
                                    device_id_type=MESH)
    pl.semaphore_wait(barrier, M * N - 1)

    def gather_start(l):
        mine = r_.gb.at[l, me]
        send(mine, mine, r_.agp_s.at[l, 0], r_.agp_r.at[l, 0], nodes=partner)
        send(mine, mine, r_.agc_s.at[l, 1], r_.agc_r.at[l, 1], nodes=2 * z_to(1) + par)
        send(mine, mine, r_.agp_s.at[l, 1], r_.agp_r.at[l, 1], nodes=2 * z_to(1) + 1 - par)
        for t in range(2, NZ):
            send(mine, mine, r_.agc_s.at[l, t], r_.agc_r.at[l, t], nodes=2 * z_to(t) + par)

    def gather_pass(l, t):
        piece = r_.gb.at[l, 2 * z_from(t) + par]
        arrive(piece, r_.agc_r.at[l, t])
        send(piece, piece, r_.agp_s.at[l, t], r_.agp_r.at[l, t], nodes=partner)

    def gather_take(l, t):
        arrive(r_.gb.at[l, 2 * z_from(t) + 1 - par], r_.agp_r.at[l, t])

    def sync_start(k, tile):
        mine = rep * N + me
        r_.st1[k, mine] = tile
        for dr in range(M):
            for d in range(N):
                if dr + d > 0:
                    send(r_.st1.at[k, mine], r_.st1.at[k, mine], r_.st1_s.at[k], r_.st1_r.at[k],
                         rep=(rep + dr) % M, nodes=(me + d) % N)

    def sync_finish(k, combine):
        arrive(r_.st1.at[k, 0 : M * N - 1], r_.st1_r.at[k])
        return unpack(combine(r_.st1[k], float(R)))

    sizes = axis_sizes(N, M)
    core, row = rep % 2, rep // 2
    places = dict(
        core=(core, lambda t: dict(rep=2 * row + t)),
        y=(row, lambda t: dict(rep=2 * t + core)),
        x=(par, lambda t: dict(nodes=2 * z + t)),
        z=(z, lambda t: dict(nodes=2 * t + par)),
        rep=(rep, lambda t: dict(rep=t)),
        nodes=(me, lambda t: dict(nodes=t)),
    )

    def reduce_step(g, step):
        name, layer, first, rows, stages = GROUPS[g]
        K = len(stages)
        gs, out = getattr(r_, f"gs_{name}").at[layer, first : first + rows], getattr(r_, f"go{g}")
        count, offset = [rows], [0]
        for axis in stages:
            count.append(count[-1] // sizes[axis])
            offset.append(offset[-1] + places[axis][0] * count[-1])
        take = lambda start, size: pl.ds(pl.multiple_of(start, 16), size)
        if 1 <= step <= K:
            k = step - 1
            got = getattr(r_, f"ga{g}_{k}")
            arrive(got, r_.ar_r.at[g, k])
            held = gs if k == 0 else getattr(r_, f"gh{g}_{k - 1}")
            index = places[stages[k]][0]
            acc = held[take(index * count[k + 1], count[k + 1])].astype(F32)
            for slot in range(sizes[stages[k]] - 1):
                acc = acc + got[slot].astype(F32)
            if step < K:
                getattr(r_, f"gh{g}_{k}")[...] = acc.astype(BF16)
            else:
                out[take(offset[K], count[K])] = acc.astype(BF16)
        elif step > K:
            k = 2 * K - step
            arrive(out.at[0 : (sizes[stages[k]] - 1) * count[k + 1]], r_.ar_r.at[g, step - 1])
        if step < K:
            held = gs if step == 0 else getattr(r_, f"gh{g}_{step - 1}")
            index, device = places[stages[step]]
            size = sizes[stages[step]]
            for d in range(1, size):
                to = (index + d) % size
                send(held.at[take(to * count[step + 1], count[step + 1])], getattr(r_, f"ga{g}_{step}").at[d - 1],
                     r_.ar_s.at[g, step], r_.ar_r.at[g, step], **device(to))
        elif step < 2 * K:
            k = 2 * K - 1 - step
            index, device = places[stages[k]]
            size = sizes[stages[k]]
            here = out.at[take(offset[k + 1], count[k + 1])]
            for d in range(1, size):
                send(here, here, r_.ar_s.at[g, step], r_.ar_r.at[g, step], **device((index + d) % size))
        else:
            pltpu.make_async_copy(out, getattr(r_, f"gout{g}"), r_.ar_l.at[g]).start()

    def reduce_drain(g):
        _, _, _, rows, stages = GROUPS[g]
        K, left = len(stages), rows
        out = getattr(r_, f"go{g}")
        for k, axis in enumerate(stages):
            left //= sizes[axis]
            for step in (k, 2 * K - 1 - k):
                sent(out.at[0 : (sizes[axis] - 1) * left], r_.ar_s.at[g, step])
        pltpu.make_async_copy(out, getattr(r_, f"gout{g}"), r_.ar_l.at[g]).wait()

    def put(buf, l, at, value):
        rows = value.shape[0]
        for c in range(value.shape[1] // 128):
            buf[l, at : at + rows] = value[:, 128 * c : 128 * (c + 1)].astype(BF16)
            at += rows
        return at

    lane_head = lax.broadcasted_iota(I32, (R, 128), 1) // HEAD_DIM

    def by_head(parts):
        out = parts[0]
        for k in range(1, HK):
            out = jnp.where(lane_head == k, parts[k], out)
        return out

    r_.meta[me] = jnp.full((8, 256), -1, I32)
    r_.meta[me, 0:1, 0:R] = r_.ids[...].reshape(1, R)
    r_.meta[me, 1:2, 0:48] = r_.halo[...].reshape(1, 48)
    for d in range(1, N):
        send(r_.meta.at[me], r_.meta.at[me], r_.meta_s.at[0], r_.meta_r.at[0], nodes=(me + d) % N)
    own_rows.wait()
    gather_start(0)

    src_row = r_.edge_src[...].reshape(1, E)
    src_row = jnp.where(src_row < R + 24, src_row, src_row + 8)
    dst_row = r_.edge_dst[...].reshape(1, E)
    src_col = jnp.broadcast_to(src_row, (128, E)).T[:, 0:1]
    dst_col = jnp.broadcast_to(dst_row, (128, E)).T[:, 0:1]
    as_mask = lambda cond: cond.astype(F32).astype(BF16)
    r_.T[...] = as_mask(dst_col == lax.broadcasted_iota(I32, (E, R), 1))
    r_.TT[...] = as_mask(dst_row == lax.broadcasted_iota(I32, (R, E), 0))
    r_.S[...] = as_mask(src_col == lax.broadcasted_iota(I32, (E, 256), 1))
    r_.ST[...] = as_mask(src_row == lax.broadcasted_iota(I32, (256, E), 0))
    loads[0].wait()
    r_.efT[...] = r_.ef[...].T
    loads[1].wait()
    for l in range(L):
        r_.ce[l] = dot(r_.ef[...], r_.we[l])
        for k in range(3):
            r_.gain[l, k : k + 1] = r_.gain_in[k, l : l + 1]
            r_.shift[l, k : k + 1] = r_.shift_in[k, l : l + 1]
    r_.xf[0] = r_.gb[0, me].astype(F32)
    r_.moff[...] = jnp.zeros((N, 8, D), F32)
    r_.move[0:1] = jnp.ones((1, D), F32)
    r_.move[1:2] = jnp.zeros((1, D), F32)
    for load in loads[2:]:
        load.wait()

    arrive(r_.meta.at[0 : N - 1], r_.meta_r.at[0])
    id_col = jnp.broadcast_to(r_.meta[me][0:1, 0:R], (128, R)).T[:, 0:1]
    id_row = jnp.concatenate([r_.meta[j][0:1, 0:R] for j in range(N)], 1)
    r_.bias[...] = jnp.where(id_col == id_row, 0.0, NEG)

    def halo_onehot(device, start):
        col = jnp.broadcast_to(r_.meta[device][1:2, 0:128], (128, 128)).T[start : start + 24, 0:1]
        hot = (col == lax.broadcasted_iota(I32, (24, R), 1)).astype(F32)
        return jnp.concatenate([hot, jnp.zeros((8, R), F32)], 0).astype(BF16)

    r_.HP[...] = halo_onehot(prev, 24)
    r_.HN[...] = halo_onehot(nxt, 0)
    r_.A[...] = as_mask(r_.meta[me][1:2, 0:64] == lax.broadcasted_iota(I32, (R, 64), 0))

    factor_exp = scale * math.log2(math.e)

    def prepare_queries(l):
        q = dot(r_.xs[l, me], r_.wqkv[l, :, :D]).astype(BF16).astype(F32)
        for hf in range(2):
            for k in range(HK):
                part = jnp.where(lane_head == k, q[:, 128 * hf : 128 * (hf + 1)], 0.0)
                r_.qm[l, hf, k * R : (k + 1) * R] = part.astype(BF16)

    def head_rows(hf, k, count=1):
        return pl.ds(pl.multiple_of((hf * HK + k) * R, 64), count * R)

    def lane_half(hf):
        return pl.ds(pl.multiple_of(hf * 128, 128), 128)

    def attention_block(l, i, middle):
        half = (zh + NB - i) % NB
        rows = pl.ds(pl.multiple_of(half * W, 128), W)
        x = r_.xs[l, pl.ds(4 * half, 4)].reshape(W, D)
        key = dot(x, r_.wqkv[l, :, D : 2 * D]).astype(BF16)
        r_.kk[l, rows] = key
        r_.kT[:, rows] = key.T
        r_.vv[l, rows] = dot(x, r_.wqkv[l, :, 2 * D :]).astype(BF16)

        def heads(hf, carry):
            lanes = lane_half(hf)
            tops, sums, outs = [], [], []
            for c in range(HK // 2):
                scores = dot(r_.qm[l, hf, 2 * c * R : 2 * (c + 1) * R], r_.kT[lanes, rows])
                for k in range(2):
                    s = scores[k * R : (k + 1) * R] + r_.bias[:, rows]
                    top = jnp.max(s, 1, keepdims=True)
                    e = jnp.exp2((s - top) * factor_exp)
                    tops.append(top)
                    sums.append(jnp.sum(e, 1, keepdims=True))
                    r_.pst[l, head_rows(hf, 2 * c + k), rows] = e.astype(BF16)
                o = dot(r_.pst[l, head_rows(hf, 2 * c, 2), rows], r_.vv[l, rows, lanes])
                outs += [o[0:R], o[R : 2 * R]]
            r_.md[i, :, lanes] = by_head([jnp.broadcast_to(v, (R, 128)) for v in tops])
            r_.ld[i, :, lanes] = by_head([jnp.broadcast_to(v, (R, 128)) for v in sums])
            r_.od[i, :, lanes] = by_head(outs)
            middle(i, hf)
            return carry

        lax.fori_loop(0, 2, heads, 0)

    def attention_end(l):
        top = r_.md[0]
        for i in range(1, NB):
            top = jnp.maximum(top, r_.md[i])
        factors = [jnp.exp2((r_.md[i] - top) * factor_exp) for i in range(NB)]
        inv = 1.0 / sum(factors[i] * r_.ld[i] for i in range(NB))
        o = jnp.zeros((R, D), F32)
        for i in range(NB):
            r_.rb[l, i] = factors[i] * inv
            o = o + factors[i] * inv * r_.od[i]
        r_.oraw[l] = o
        ob = o.astype(BF16)
        r_.ob[l] = ob
        t1 = r_.xf[l] + dot(ob, r_.wo[l])
        r_.z1[l] = t1
        mean1 = col_sum(t1) / R
        return mean1, col_sum((t1 - mean1) * (t1 - mean1))

    def convolution(l):
        xs = r_.xs
        xb = xs[l, me]
        r_.xe[l, 0:R] = xb
        r_.xe[l, R : R + 32] = dot(r_.HP[...], xs[l, prev]).astype(BF16)
        r_.xe[l, R + 32 : R + 64] = dot(r_.HN[...], xs[l, nxt]).astype(BF16)
        xe = r_.xe[l]
        tab_b = dot(xe, r_.wp[l, :, D : 2 * D]).astype(BF16)
        tab_e = dot(xe, r_.wp[l, :, 3 * D :]).astype(BF16)
        pa = dot(xb, r_.wp[l, :, 0:D])
        pd = dot(xb, r_.wp[l, :, 2 * D : 3 * D])
        bs = dot(r_.S[...], tab_b)
        r_.bs[l] = bs.astype(BF16)
        gate = sigmoid(select_rows(r_.T[...], pd) + dot(r_.S[...], tab_e) + r_.ce[l])
        r_.gate[l] = gate
        num = select_rows(r_.TT[...], gate * bs)
        den = select_rows(r_.TT[...], gate)
        r_.num[l] = num
        r_.den[l] = den
        msg = pa + num / (den + GATE_EPS)
        r_.z0[l] = msg

    def forward(l, carry):
        def ready(js):
            for j in js:
                moved = (r_.gb[l, j].astype(F32) + r_.moff[j, 0:1]) * r_.move[0:1] + r_.move[1:2]
                r_.xs[l, j] = moved.astype(BF16)

        r_.xs[l, me] = r_.xf[l].astype(BF16)
        prepare_queries(l)
        arrive(r_.gb.at[l, 2 * z_from(1) + par], r_.agc_r.at[l, 1])
        gather_take(l, 0)
        gather_take(l, 1)
        ready([partner, 2 * z_from(1) + par, 2 * z_from(1) + 1 - par])

        def middle(i, hf):
            when((i == 0) & (hf == 0), *[functools.partial(gather_pass, l, t) for t in range(2, NZ)])

        def block(i, carry):
            attention_block(l, i, middle)

            @pl.when(i == 0)
            def _():
                for t in range(2, NZ):
                    gather_take(l, t)
                ready([2 * z_from(t) + p for t in range(2, NZ) for p in range(2)])
                convolution(l)

            return carry

        lax.fori_loop(0, NB, block, 0)
        mean1, sq1 = attention_end(l)
        msg = r_.z0[l]
        mean0 = col_sum(msg) / R
        sq0 = col_sum((msg - mean0) * (msg - mean0))
        sync_start(2 * l, pack(mean0, mean1, sq0, sq1))
        mean0, mean1, sq0, sq1 = sync_finish(2 * l, combine_pair)
        inv0 = lax.rsqrt(sq0 / total + NORM_EPS)
        inv1 = lax.rsqrt(sq1 / total + NORM_EPS)
        r_.iv[l, 0:1] = inv0
        r_.iv[l, 1:2] = inv1
        z0 = (r_.z0[l] - mean0) * inv0
        z1 = (r_.z1[l] - mean1) * inv1
        r_.z0[l] = z0
        r_.z1[l] = z1
        n0 = z0 * r_.gain[l, 0:1] + r_.shift[l, 0:1]
        mix = r_.xf[l] + n0 * sigmoid(n0) + z1 * r_.gain[l, 1:2] + r_.shift[l, 1:2]
        mb = mix.astype(BF16)
        r_.mb[l] = mb
        u = dot(mb, r_.wu[l])
        r_.u[l] = u
        g = (u * sigmoid(u)).astype(BF16)
        r_.g[l] = g
        y = mix + dot(g, r_.wd[l])
        r_.z2[l] = y
        mean = col_sum(y) / R
        cent = y - mean
        k = 2 * l + 1
        dy = r_.cot[...].astype(F32)
        sync_start(k, pack(mean, col_sum(dy), col_sum(cent * cent), col_sum(dy * cent)))

        @pl.when(l < L - 1)
        def _():
            r_.gb[l + 1, me] = cent.astype(BF16)
            gather_start(l + 1)

        tot_mean, dy_sum, tot_sq, dy_cent = sync_finish(k, combine_last)
        inv2 = lax.rsqrt(tot_sq / total + NORM_EPS)
        r_.iv[l, 2:3] = inv2
        z2 = (r_.z2[l] - tot_mean) * inv2
        r_.z2[l] = z2
        gain, shift = r_.gain[l, 2:3], r_.shift[l, 2:3]
        r_.xf[l + 1] = z2 * gain + shift
        r_.gshift[l, 2:3] = dy_sum
        r_.ggain[l, 2:3] = dy_cent * inv2
        for j in range(N):
            tile = r_.st1[k, rep * N + j]
            r_.moff[j, 0:1] = jnp.concatenate([tile[0:1], tile[1:2]], 1) - tot_mean
        r_.move[0:1] = inv2 * gain
        r_.move[1:2] = shift
        return carry

    lax.fori_loop(0, L, forward, 0)
    act_copy = pltpu.make_async_copy(r_.xf.at[L], r_.out_act, r_.store.at[0])
    act_copy.start()

    def back_feed_forward(l, k):
        s2, g2 = r_.gshift[l, 2:3], r_.ggain[l, 2:3]
        d3 = r_.gain[l, 2:3] * r_.iv[l, 2:3] * (r_.dy[...] - s2 / total - r_.z2[l] * (g2 / total))
        db = d3.astype(BF16)
        dub = (dot_nt(db, r_.wd[l]) * silu_slope(r_.u[l])).astype(BF16)
        dmix = d3 + dot_nt(dub, r_.wu[l])
        r_.dmix[...] = dmix
        n0 = r_.z0[l] * r_.gain[l, 0:1] + r_.shift[l, 0:1]
        gy0 = dmix * silu_slope(n0)
        sync_start(k, pack(col_sum(dmix), col_sum(dmix * r_.z1[l]), col_sum(gy0), col_sum(gy0 * r_.z0[l])))
        at = put(r_.gs_early, l, 512, dot_tn(r_.mb[l], dub))
        put(r_.gs_early, l, at, dot_tn(r_.g[l], db))
        r_.vT[...] = r_.vv[l].T
        r_.xeT[...] = r_.xe[l].T
        for hf in range(2):
            r_.qmT[hf] = r_.qm[l, hf].T

    def back_norms(l, k):
        s1, g1, s0, g0 = sync_finish(k, combine_sum)
        r_.gshift[l, 1:2] = s1
        r_.ggain[l, 1:2] = g1
        r_.gshift[l, 0:1] = s0
        r_.ggain[l, 0:1] = g0
        dmix = r_.dmix[...]
        d2 = r_.gain[l, 1:2] * r_.iv[l, 1:2] * (dmix - s1 / total - r_.z1[l] * (g1 / total))
        dab = d2.astype(BF16)
        r_.dxo[...] = dmix + d2
        r_.dob[...] = dot_nt(dab, r_.wo[l]).astype(BF16).astype(F32)
        put(r_.gs_early, l, 0, dot_tn(r_.ob[l], dab))
        r_.gkv[...] = jnp.zeros((2 * D, D), F32)
        r_.dq[...] = jnp.zeros((R, D), F32)

    def back_attention_block(l, i, between):
        t1 = (i + 1) % NB
        half = (zh + t1) % NB
        rows = pl.ds(pl.multiple_of(half * W, 128), W)

        def heads(hf, carry):
            lanes = lane_half(hf)
            dos = r_.dob[:, lanes] * r_.rb[l, (NB - t1) % NB, :, lanes]
            prod = dos * r_.oraw[l, :, lanes]
            for k in range(HK):
                r_.dom[k * R : (k + 1) * R] = jnp.where(lane_head == k, dos, 0.0).astype(BF16)
            parts = []
            for c in range(HK // 2):
                both = slice(2 * c * R, 2 * (c + 1) * R)
                dp = dot(r_.dom[both], r_.vT[lanes, rows])
                for k in range(2):
                    h = 2 * c + k
                    delta = jnp.sum(jnp.where(lane_head == h, prod, 0.0), 1, keepdims=True)
                    ds = r_.pst[l, head_rows(hf, h), rows].astype(F32) * (dp[k * R : (k + 1) * R] - delta)
                    r_.dss[h * R : (h + 1) * R] = ds.astype(BF16)
                part = dot(r_.dss[both], r_.kk[l, rows, lanes])
                parts += [part[0:R], part[R : 2 * R]]
            r_.dq[:, lanes] += by_head(parts)
            dk = dot(r_.qmT[hf], r_.dss[...]) * scale
            r_.dkv[pl.ds(pl.multiple_of(hf * 128, 128), 128)] = dk.astype(BF16)
            dv = dot(r_.dom[...].T, r_.pst[l, head_rows(hf, 0, HK), rows])
            r_.dkv[pl.ds(pl.multiple_of(D + hf * 128, 128), 128)] = dv.astype(BF16)
            between(i, hf)
            return carry

        lax.fori_loop(0, 2, heads, 0)
        dx = dot(r_.wqkv[l, :, D:], r_.dkv[...]).T
        r_.dxs[l, pl.ds(2 * half, 2)] = dx.astype(BF16).reshape(2, 2, R, D)

        @pl.when(i < NB - 1)
        def _():
            for low in range(2):
                zb = 2 * half + low
                send(r_.dxs.at[l, zb, 1 - par], r_.rs1.at[l, zb],
                     r_.rsp_s.at[l, 2 * i + low], r_.rsp_r.at[l, 2 * i + low], nodes=partner)

        @pl.when(i == NB - 1)
        def _():
            near = z_to(1)
            send(r_.dxs.at[l, z, 1 - par], r_.ro.at[l, 0], r_.ro_s.at[l, 0], r_.ro_r.at[l, 0], nodes=partner)
            send(r_.dxs.at[l, near, par], r_.ro.at[l, 1], r_.ro_s.at[l, 1], r_.ro_r.at[l, 1], nodes=2 * near + par)
            send(r_.dxs.at[l, near, 1 - par], r_.ro.at[l, 2], r_.ro_s.at[l, 2], r_.ro_r.at[l, 2],
                 nodes=2 * near + 1 - par)

        r_.gkv[...] += dot(r_.dkv[...], r_.xs[l, pl.ds(4 * half, 4)].reshape(W, D))

    def pass_on(l, i, t):
        zb = z_to(t)
        arrive(r_.rs1.at[l, zb], r_.rsp_r.at[l, 2 * i + zb % 2])
        both = r_.dxs[l, zb, par].astype(F32) + r_.rs1[l, zb].astype(F32)
        r_.cs[l, zb] = both.astype(BF16)
        send(r_.cs.at[l, zb], r_.rs2.at[l, z], r_.rsc_s.at[l, t], r_.rsc_r.at[l, t], nodes=2 * zb + par)

    def back_convolution(l):
        s0, g0 = r_.gshift[l, 0:1], r_.ggain[l, 0:1]
        inv_den = 1.0 / (r_.den[l] + GATE_EPS)
        n0 = r_.z0[l] * r_.gain[l, 0:1] + r_.shift[l, 0:1]
        gy0 = r_.dmix[...] * silu_slope(n0)
        dm = r_.gain[l, 0:1] * r_.iv[l, 0:1] * (gy0 - s0 / total - r_.z0[l] * (g0 / total))
        dnum = dm * inv_den
        dden = -dnum * r_.num[l] * inv_den
        dnum_e = select_rows(r_.T[...], dnum)
        dden_e = select_rows(r_.T[...], dden)
        gate = r_.gate[l]
        dgp = (dnum_e * r_.bs[l].astype(F32) + dden_e) * gate * (1.0 - gate)
        r_.dce[...] = dgp.astype(BF16)
        dpb = select_rows(r_.ST[...], dnum_e * gate).astype(BF16)
        dpe = select_rows(r_.ST[...], dgp).astype(BF16)
        dpd = select_rows(r_.TT[...], dgp).astype(BF16)
        dmb = dm.astype(BF16)
        dxe = dot_nt(dpb, r_.wp[l, :, D : 2 * D]) + dot_nt(dpe, r_.wp[l, :, 3 * D :])
        r_.hs[l, 0] = dxe[R : R + 32].astype(BF16)
        r_.hs[l, 1] = dxe[R + 32 : R + 64].astype(BF16)
        send(r_.hs.at[l, 0], r_.hr.at[l, 1], r_.hal_s.at[l, 0], r_.hal_r.at[l, 0], nodes=prev)
        send(r_.hs.at[l, 1], r_.hr.at[l, 0], r_.hal_s.at[l, 1], r_.hal_r.at[l, 1], nodes=nxt)
        r_.dxo[...] += (
            dxe[0:R]
            + dot_nt(dmb, r_.wp[l, :, 0:D])
            + dot_nt(dpd, r_.wp[l, :, 2 * D : 3 * D])
        )
        r_.dproj[0, 0:R] = dmb
        r_.dproj[1] = dpb
        r_.dproj[2, 0:R] = dpd
        r_.dproj[3] = dpe

    def conv_weight_grads(l):
        at = 0
        for c in range(4):
            width = R if c % 2 == 0 else 256
            at = put(r_.gs_conv, l, at, dot(r_.xeT[:, 0:width], r_.dproj[c, 0:width]))
        put(r_.gs_conv, l, at, dot(r_.efT[...], r_.dce[...]))

    def back_input(l):
        dx = r_.dxo[...]
        dx = dx + r_.dxs[l, z, par].astype(F32)
        for slot in range(3):
            arrive(r_.ro.at[l, slot], r_.ro_r.at[l, slot])
            dx = dx + r_.ro[l, slot].astype(F32)
        for t in range(2, NZ):
            c = z_from(t)
            arrive(r_.rs2.at[l, c], r_.rsc_r.at[l, t])
            dx = dx + r_.rs2[l, c].astype(F32)
        arrive(r_.hr.at[l, 0], r_.hal_r.at[l, 1])
        arrive(r_.hr.at[l, 1], r_.hal_r.at[l, 0])
        back = jnp.concatenate(
            [r_.hr[l, 0].astype(F32)[0:24], r_.hr[l, 1].astype(F32)[0:24], jnp.zeros((16, D), F32)], 0
        )
        return dx + dot(r_.A[...], back.astype(BF16))

    r_.dy[...] = r_.cot[...].astype(F32)

    E1, C1, Q1, E0, C0, QK0, V0 = range(len(GROUPS))

    def steps(*pairs):
        return [functools.partial(reduce_step, g, k) for g, k in pairs]

    def backward(b, carry):
        l = L - 1 - b
        first, last = b == 0, b == L - 1
        k = 4 + 2 * b
        back_feed_forward(l, k)
        when(last, *steps((C1, 4), (Q1, 1), (E1, 5)))
        back_norms(l, k)
        when(first, *steps((E1, 0)))
        when(last, *steps((E0, 0), (Q1, 2), (E1, 6), (C1, 5)))
        back_convolution(l)
        conv_weight_grads(l)
        when(first, *steps((E1, 1), (C1, 0)))
        when(last, *steps((E0, 1), (C0, 0), (Q1, 3), (C1, 6)))

        def between(i, hf):
            when(first & (i == 0) & (hf == 0), *steps((C1, 1)))
            when(first & (i == 0) & (hf == 1), *steps((E1, 2)))
            when(first & (i == 1) & (hf == 0), *steps((C1, 2)))
            when(first & (i == 1) & (hf == 1), *steps((E1, 3)))
            when(last & (i == 0) & (hf == 0), *steps((C0, 1)))
            when(last & (i == 0) & (hf == 1), *steps((E0, 2), (Q1, 4)))
            when(last & (i == 1) & (hf == 0), *steps((C0, 2)))
            when(last & (i == 1) & (hf == 1), *steps((E0, 3), (Q1, 5)))
            for t in range(2, NZ):
                when((i == 1) & (hf == 0), functools.partial(pass_on, l, 0, t))

        def block(i, carry):
            back_attention_block(l, i, between)
            return carry

        lax.fori_loop(0, NB, block, 0)
        dqb = (r_.dq[...] * scale).astype(BF16)
        r_.dxo[...] += dot_nt(dqb, r_.wqkv[l, :, 0:D])
        at = put(r_.gs_qkv, l, 0, dot(r_.xeT[:, 0:R], dqb))
        put(r_.gs_qkv, l, at, r_.gkv[...].T)
        when(first, *steps((Q1, 0)))

        @pl.when(first)
        def _():
            dx = back_input(l)
            r_.dy[...] = dx
            below = L - 2
            zero_row = jnp.zeros((1, D), F32)
            sync_start(5, pack(col_sum(dx), col_sum(dx * r_.z2[below]), zero_row, zero_row))
            for step in steps((C1, 3), (E1, 4)):
                step()
            s2, g2, _, _ = sync_finish(5, combine_sum)
            r_.gshift[below, 2:3] = s2
            r_.ggain[below, 2:3] = g2

        return carry

    lax.fori_loop(0, L, backward, 0)
    for step in steps((QK0, 0), (V0, 0), (C0, 3), (E0, 4), (Q1, 6), (V0, 1), (QK0, 1)):
        step()
    r_.dy[...] = back_input(0)
    in_copy = pltpu.make_async_copy(r_.dy, r_.grad_in, r_.store.at[1])
    in_copy.start()
    for step in steps(
        (C0, 4), (E0, 5), (V0, 2), (QK0, 2),
        (C0, 5), (E0, 6), (V0, 3), (QK0, 3),
        (C0, 6), (V0, 4), (QK0, 4),
    ):
        step()
    for l in range(L):
        for k in range(3):
            r_.ggain_out[k, l : l + 1] = r_.ggain[l, k : k + 1]
            r_.gshift_out[k, l : l + 1] = r_.gshift[l, k : k + 1]
    for g in range(len(GROUPS)):
        reduce_drain(g)
    sent(r_.meta.at[0 : N - 1], r_.meta_s.at[0])
    for k in range(SYNCS):
        sent(r_.st1.at[k, 0 : M * N - 1], r_.st1_s.at[k])
    for l in range(L):
        for t in range(NZ):
            sent(r_.gb.at[l, 0], r_.agp_s.at[l, t])
            if t > 0:
                sent(r_.gb.at[l, 0], r_.agc_s.at[l, t])
            if t > 1:
                sent(r_.rs1.at[l, 0], r_.rsc_s.at[l, t])
        for slot in range(2 * (NB - 1)):
            sent(r_.rs1.at[l, 0], r_.rsp_s.at[l, slot])
        for slot in range(3):
            sent(r_.ro.at[l, 0], r_.ro_s.at[l, slot])
        for side in range(2):
            sent(r_.hs.at[l, 0], r_.hal_s.at[l, side])
    act_copy.wait()
    in_copy.wait()


def finish_kernel(act_h, gin_h, *refs):
    n = len(GROUPS)
    held, (ggain_h, gshift_h), refs = refs[:n], refs[n : n + 2], refs[n + 2 :]
    act_o, gin_o, proj_o, edge_o, qkv_o, out_o, up_o, down_o, ggain_o, gshift_o = refs[:10]
    summed, refs = refs[10 : 10 + n], refs[10 + n :]
    act, gin, proj, edge, qkv, out, up, down, in_sem, out_sem = refs
    loads = [
        pltpu.make_async_copy(src, dst, in_sem.at[i])
        for i, (src, dst) in enumerate(zip(held + (act_h, gin_h), summed + (act, gin), strict=True))
    ]
    for load in loads:
        load.start()
    ggain_o[...] = ggain_h[...]
    gshift_o[...] = gshift_h[...]
    stores = []

    def store(src, dst):
        copy = pltpu.make_async_copy(src, dst, out_sem.at[len(stores)])
        copy.start()
        stores.append(copy)

    def widen(dst, l, g, at, first=0, last=None):
        rows = dst.shape[1]
        for c in range(first, dst.shape[2] // 128 if last is None else last):
            dst[l, :, 128 * c : 128 * (c + 1)] = summed[g][at : at + rows].astype(F32)
            at += rows
        return at

    for g, (name, l, first, rows, _) in enumerate(GROUPS):
        loads[g].wait()
        if name == "early":
            at = widen(out, l, g, 0)
            store(out.at[l], out_o.at[l])
            at = widen(up, l, g, at)
            store(up.at[l], up_o.at[l])
            widen(down, l, g, at)
            store(down.at[l], down_o.at[l])
        elif name == "conv":
            at = widen(proj, l, g, 0)
            store(proj.at[l], proj_o.at[l])
            widen(edge, l, g, at)
            store(edge.at[l], edge_o.at[l])
        else:
            widen(qkv, l, g, 0, first // 256, (first + rows) // 256)
            if first + rows == 1536:
                store(qkv.at[l], qkv_o.at[l])
    for i, (src, dst) in enumerate(((act, act_o), (gin, gin_o))):
        loads[n + i].wait()
        store(src, dst)
    for copy in stores:
        copy.wait()


def fused_device(
    N, M, node_input, edge_feat, graph_ids, edge_src, edge_dst, halo_send, w_proj, w_edge, w_qkv,
    w_out, w_up, w_down, norm_gain, norm_shift, cotangent,
):
    R, D = node_input.shape
    E = edge_feat.shape[0]
    L = w_proj.shape[0]
    names = scratch_list(N, M, L, R, E)
    vmem = pl.BlockSpec(memory_space=pltpu.VMEM)
    hbm = pl.BlockSpec(memory_space=pltpu.HBM)
    shape = jax.ShapeDtypeStruct
    rows = shape((R, D), F32)
    norm = shape((3, L, D), F32)
    groups = [shape((rows_g, 128), BF16) for _, _, _, rows_g, _ in GROUPS]
    outs = pl.pallas_call(
        functools.partial(kernel, N, M, L, tuple(names)),
        out_shape=[rows, rows, *groups, norm, norm],
        in_specs=[hbm] + [vmem] * 4 + [hbm] * 7 + [vmem] * 2 + [hbm],
        out_specs=[hbm] * (2 + len(GROUPS)) + [vmem] * 2,
        scratch_shapes=list(names.values()),
        compiler_params=pltpu.CompilerParams(
            collective_id=0, has_side_effects=True, vmem_limit_bytes=60 << 20
        ),
        name="layers",
    )(node_input, graph_ids, edge_src, edge_dst, halo_send, edge_feat, w_proj, w_edge, w_qkv, w_out, w_up,
      w_down, norm_gain.transpose(1, 0, 2), norm_shift.transpose(1, 0, 2), cotangent)
    weights = [shape(w.shape, F32) for w in (w_proj, w_edge, w_qkv, w_out, w_up, w_down)]
    results = pl.pallas_call(
        finish_kernel,
        out_shape=[rows, rows, *weights, norm, norm],
        in_specs=[hbm] * (2 + len(GROUPS)) + [vmem] * 2,
        out_specs=[hbm] * 8 + [vmem] * 2,
        scratch_shapes=[pltpu.VMEM(s.shape, s.dtype) for s in (*groups, rows, rows, *weights)]
        + [pltpu.SemaphoreType.DMA((len(GROUPS) + 2,)), pltpu.SemaphoreType.DMA((14,))],
        compiler_params=pltpu.CompilerParams(vmem_limit_bytes=60 << 20),
        name="gradients",
    )(*outs)
    ggain, gshift = results[8].transpose(1, 0, 2), results[9].transpose(1, 0, 2)
    return (*results[:8], ggain, gshift)


BLOCK_CAP = 2048


def extended_2(block, sides, width):
    for axis, dim in sides:
        count = lax.axis_size(axis)
        forward = [(i, i + 1) for i in range(count - 1)]
        forward.append((count - 1, 0))
        backward = [(target, source) for source, target in forward]
        low = lax.ppermute(
            lax.slice_in_dim(block, block.shape[dim] - width, None, axis=dim), axis, forward
        )
        high = lax.ppermute(lax.slice_in_dim(block, 0, width, axis=dim), axis, backward)
        block = jnp.concatenate([low, block, high], axis=dim)
    return block


def block_length(total_rows, upper_limit):
    for length in range(min(total_rows, upper_limit), 0, -1):
        if total_rows % length == 0:
            return length
    return 1


def outer_product(left, right):
    return lax.dot_general(
        left, right, (((0,), (0,)), ((), ())), preferred_element_type=jnp.float32
    )


def times_transposed(left, weight):
    return lax.dot_general(
        left, weight, (((1,), (1,)), ((), ())), preferred_element_type=jnp.float32
    )


def forward_product(left, weight):
    return jnp.dot(left, weight, preferred_element_type=jnp.float32)


def silu_slope_plain(inputs):
    logistic = jax.nn.sigmoid(inputs)
    return logistic * (1.0 + inputs * (1.0 - logistic))


def normalize(inputs, gain_row, shift_row, node_total):
    batch_mean = lax.psum(jnp.sum(inputs, 0), ("nodes", "rep")) / node_total
    centred = inputs - batch_mean
    batch_var = lax.psum(jnp.sum(centred * centred, 0), ("nodes", "rep")) / node_total
    inv_std = lax.rsqrt(batch_var + NORM_EPS)
    standard = (inputs - batch_mean) * inv_std
    return (standard * gain_row + shift_row, standard, inv_std)


def normalize_back(grad_out, standard, inv_std, gain_row, node_total):
    shift_grad, gain_grad = lax.psum(
        (jnp.sum(grad_out, 0), jnp.sum(grad_out * standard, 0)), ("nodes", "rep")
    )
    grad_in = (
        gain_row
        * inv_std
        * (grad_out - shift_grad / node_total - standard * gain_grad / node_total)
    )
    return (grad_in, gain_grad, shift_grad)


def exchange_sources(outgoing):
    halo_rows = outgoing.shape[0] // 2
    grown = extended_2(outgoing, (("nodes", 0),), halo_rows)
    return jnp.concatenate([grown[:halo_rows], grown[3 * halo_rows :]], 0)


def return_sources(incoming_grad):
    halo_rows = incoming_grad.shape[0] // 2
    grown = extended_2(incoming_grad.astype(jnp.bfloat16), (("nodes", 0),), halo_rows).astype(
        incoming_grad.dtype
    )
    return jnp.concatenate([grown[:halo_rows], grown[3 * halo_rows :]], 0)


def attend_forward(query_rows, key_rows, value_rows, local_graphs, group_graphs):
    row_count = query_rows.shape[0]
    score_scale = HEAD_DIM ** (-0.5)
    queries = query_rows.reshape(row_count, HEADS, HEAD_DIM)

    def add_piece(carried, kv_piece, first_row):
        key_piece, value_piece = kv_piece
        piece_rows = key_piece.shape[0]
        block_len = block_length(piece_rows, BLOCK_CAP)

        def add_block(block_state, block_index):
            row_max, row_sum, accumulated = block_state
            block_start = block_index * block_len
            key_block = lax.dynamic_slice_in_dim(key_piece, block_start, block_len, 0).reshape(
                block_len, HEADS, HEAD_DIM
            )
            value_block = lax.dynamic_slice_in_dim(value_piece, block_start, block_len, 0).reshape(
                block_len, HEADS, HEAD_DIM
            )
            key_graphs = lax.dynamic_slice_in_dim(
                group_graphs, first_row + block_start, block_len, 0
            )
            same_graph = (local_graphs[:, None] == key_graphs[None, :])[None]
            scores = (
                jnp.einsum("qhd,khd->hqk", queries, key_block, preferred_element_type=jnp.float32)
                * score_scale
            )
            scores = jnp.where(same_graph, scores, NEG)
            new_max = jnp.maximum(row_max, jnp.max(scores, 2))
            weights = jnp.where(same_graph, jnp.exp(scores - new_max[:, :, None]), 0.0)
            factor = jnp.exp(row_max - new_max)
            row_sum = row_sum * factor + jnp.sum(weights, 2)
            contrib = jnp.einsum(
                "hqk,khd->qhd",
                weights.astype(jnp.bfloat16),
                value_block,
                preferred_element_type=jnp.float32,
            )
            accumulated = accumulated * jnp.transpose(factor)[:, :, None] + contrib
            return ((new_max, row_sum, accumulated), None)

        carried, _ = lax.scan(add_block, carried, jnp.arange(piece_rows // block_len))
        return carried

    start_state = (
        jnp.full((HEADS, row_count), NEG, jnp.float32),
        jnp.zeros((HEADS, row_count), jnp.float32),
        jnp.zeros((row_count, HEADS, HEAD_DIM), jnp.float32),
    )
    row_max, row_sum, accumulated = add_piece(
        start_state,
        (
            lax.all_gather(key_rows, "nodes", axis=0, tiled=True),
            lax.all_gather(value_rows, "nodes", axis=0, tiled=True),
        ),
        jnp.int32(0),
    )
    attn_raw = accumulated / jnp.transpose(row_sum)[:, :, None]
    log_sum = row_max + jnp.log(row_sum)
    return (attn_raw, log_sum)


def attend_backward(
    query_rows, key_rows, value_rows, grad_low, attn_raw, log_sum, local_graphs, group_graphs
):
    row_count = query_rows.shape[0]
    model_width = HEADS * HEAD_DIM
    score_scale = HEAD_DIM ** (-0.5)
    queries = query_rows.reshape(row_count, HEADS, HEAD_DIM)
    grad_heads = grad_low.reshape(row_count, HEADS, HEAD_DIM)
    row_delta = jnp.einsum("qhd,qhd->hq", grad_heads.astype(jnp.float32), attn_raw)

    def score_block(key_block, value_block, key_graphs):
        same_graph = (local_graphs[:, None] == key_graphs[None, :])[None]
        scores = (
            jnp.einsum("qhd,khd->hqk", queries, key_block, preferred_element_type=jnp.float32)
            * score_scale
        )
        attn_weights = jnp.exp(jnp.where(same_graph, scores - log_sum[:, :, None], NEG))
        grad_weights = jnp.einsum(
            "qhd,khd->hqk", grad_heads, value_block, preferred_element_type=jnp.float32
        )
        grad_scores = (attn_weights * (grad_weights - row_delta[:, :, None])).astype(jnp.bfloat16)
        return (attn_weights, grad_scores)

    def key_terms(attn_weights, grad_scores, block_len):
        grad_keys = (
            jnp.einsum("hqk,qhd->khd", grad_scores, queries, preferred_element_type=jnp.float32)
            * score_scale
        )
        grad_values = jnp.einsum(
            "hqk,qhd->khd",
            attn_weights.astype(jnp.bfloat16),
            grad_heads,
            preferred_element_type=jnp.float32,
        )
        return jnp.concatenate(
            [
                grad_keys.reshape(block_len, model_width),
                grad_values.reshape(block_len, model_width),
            ],
            1,
        )

    def query_term(grad_scores, key_block):
        return (
            jnp.einsum("hqk,khd->qhd", grad_scores, key_block, preferred_element_type=jnp.float32)
            * score_scale
        )

    group_rows = group_graphs.shape[0]

    def add_piece(carried, kv_piece, first_row):
        key_piece, value_piece = kv_piece
        piece_rows = key_piece.shape[0]
        block_len = block_length(piece_rows, BLOCK_CAP)

        def add_block(block_state, block_index):
            grad_query, buffer = block_state
            block_start = block_index * block_len
            key_block = lax.dynamic_slice_in_dim(key_piece, block_start, block_len, 0).reshape(
                block_len, HEADS, HEAD_DIM
            )
            value_block = lax.dynamic_slice_in_dim(value_piece, block_start, block_len, 0).reshape(
                block_len, HEADS, HEAD_DIM
            )
            place = first_row + block_start
            key_graphs = lax.dynamic_slice_in_dim(group_graphs, place, block_len, 0)
            attn_weights, grad_scores = score_block(key_block, value_block, key_graphs)
            grad_query = grad_query + query_term(grad_scores, key_block)
            block_terms = key_terms(attn_weights, grad_scores, block_len)
            current = lax.dynamic_slice_in_dim(buffer, place, block_len, 0)
            buffer = lax.dynamic_update_slice_in_dim(buffer, current + block_terms, place, 0)
            return ((grad_query, buffer), None)

        carried, _ = lax.scan(add_block, carried, jnp.arange(piece_rows // block_len))
        return carried

    start_state = (
        jnp.zeros((row_count, HEADS, HEAD_DIM), jnp.float32),
        jnp.zeros((group_rows, 2 * model_width), jnp.float32),
    )
    grad_query, buffer = add_piece(
        start_state,
        (
            lax.all_gather(key_rows, "nodes", axis=0, tiled=True),
            lax.all_gather(value_rows, "nodes", axis=0, tiled=True),
        ),
        jnp.int32(0),
    )
    grad_kv = lax.psum_scatter(buffer, "nodes", scatter_dimension=0, tiled=True)
    return (
        grad_query.reshape(row_count, model_width),
        grad_kv[:, :model_width],
        grad_kv[:, model_width:],
    )


def layer_forward(
    hidden, params, edge_feat, edge_src, edge_dst, halo_send, local_graphs, group_graphs, node_total
):
    w_proj, w_edge, w_qkv, w_out, w_up, w_down, norm_gains, norm_shifts = params
    row_count, model_width = hidden.shape
    hidden_low = hidden.astype(jnp.bfloat16)
    projected = forward_product(hidden_low, w_proj)
    self_term = projected[:, :model_width]
    dest_term = projected[:, 2 * model_width : 3 * model_width]
    source_rows = jnp.concatenate(
        [projected[:, model_width : 2 * model_width], projected[:, 3 * model_width :]], 1
    ).astype(jnp.bfloat16)
    incoming = exchange_sources(source_rows[halo_send])
    extended = jnp.concatenate([source_rows, incoming], 0)
    edge_rows = extended[edge_src].astype(jnp.float32)
    source_b = edge_rows[:, :model_width]
    source_e = edge_rows[:, model_width:]
    edge_proj = forward_product(edge_feat, w_edge)
    gating = jax.nn.sigmoid(dest_term[edge_dst] + source_e + edge_proj)
    numerator = jax.ops.segment_sum(gating * source_b, edge_dst, row_count)
    denominator = jax.ops.segment_sum(gating, edge_dst, row_count)
    message = self_term + numerator / (denominator + GATE_EPS)
    normed_one, standard_one, inv_one = normalize(
        message, norm_gains[0], norm_shifts[0], node_total
    )
    local_out = hidden + jax.nn.silu(normed_one)
    qkv_low = forward_product(hidden_low, w_qkv).astype(jnp.bfloat16)
    query_rows = qkv_low[:, :model_width]
    key_rows = qkv_low[:, model_width : 2 * model_width]
    value_rows = qkv_low[:, 2 * model_width :]
    attn_raw, log_sum = attend_forward(query_rows, key_rows, value_rows, local_graphs, group_graphs)
    attn_low = attn_raw.reshape(row_count, model_width).astype(jnp.bfloat16)
    attn_proj = forward_product(attn_low, w_out)
    normed_two, standard_two, inv_two = normalize(
        hidden + attn_proj, norm_gains[1], norm_shifts[1], node_total
    )
    mixed = local_out + normed_two
    mixed_low = mixed.astype(jnp.bfloat16)
    up_proj = forward_product(mixed_low, w_up)
    activated = jax.nn.silu(up_proj).astype(jnp.bfloat16)
    down_proj = forward_product(activated, w_down)
    normed_three, standard_three, inv_three = normalize(
        mixed + down_proj, norm_gains[2], norm_shifts[2], node_total
    )
    saved = (
        hidden_low,
        source_b,
        gating,
        numerator,
        denominator,
        normed_one,
        standard_one,
        inv_one,
        query_rows,
        key_rows,
        value_rows,
        attn_raw,
        log_sum,
        attn_low,
        standard_two,
        inv_two,
        mixed_low,
        up_proj,
        activated,
        standard_three,
        inv_three,
    )
    return (normed_three, saved)


def layer_backward(
    grad_out,
    params,
    saved,
    edge_feat,
    edge_src,
    edge_dst,
    halo_send,
    local_graphs,
    group_graphs,
    node_total,
):
    w_proj, w_edge, w_qkv, w_out, w_up, w_down, norm_gains, norm_shifts = params
    (
        hidden_low,
        source_b,
        gating,
        numerator,
        denominator,
        normed_one,
        standard_one,
        inv_one,
        query_rows,
        key_rows,
        value_rows,
        attn_raw,
        log_sum,
        attn_low,
        standard_two,
        inv_two,
        mixed_low,
        up_proj,
        activated,
        standard_three,
        inv_three,
    ) = saved
    row_count, model_width = grad_out.shape
    grad_three, gain_three, shift_three = normalize_back(
        grad_out, standard_three, inv_three, norm_gains[2], node_total
    )
    down_grad = grad_three.astype(jnp.bfloat16)
    grad_w_down = outer_product(activated, down_grad)
    up_grad = (times_transposed(down_grad, w_down) * silu_slope_plain(up_proj)).astype(jnp.bfloat16)
    grad_w_up = outer_product(mixed_low, up_grad)
    grad_mixed = grad_three + times_transposed(up_grad, w_up)
    grad_two, gain_two, shift_two = normalize_back(
        grad_mixed, standard_two, inv_two, norm_gains[1], node_total
    )
    out_grad = grad_two.astype(jnp.bfloat16)
    grad_w_out = outer_product(attn_low, out_grad)
    attn_grad = times_transposed(out_grad, w_out).astype(jnp.bfloat16)
    grad_query, grad_key, grad_value = attend_backward(
        query_rows, key_rows, value_rows, attn_grad, attn_raw, log_sum, local_graphs, group_graphs
    )
    qkv_grad = jnp.concatenate([grad_query, grad_key, grad_value], 1).astype(jnp.bfloat16)
    grad_w_qkv = outer_product(hidden_low, qkv_grad)
    grad_message, gain_one, shift_one = normalize_back(
        grad_mixed * silu_slope_plain(normed_one), standard_one, inv_one, norm_gains[0], node_total
    )
    shifted = denominator + GATE_EPS
    grad_numer = grad_message / shifted
    grad_denom = -grad_message * numerator / (shifted * shifted)
    numer_edge = grad_numer[edge_dst]
    grad_gate = numer_edge * source_b + grad_denom[edge_dst]
    grad_pre_edge = grad_gate * gating * (1.0 - gating)
    edge_grad = grad_pre_edge.astype(jnp.bfloat16)
    grad_w_edge = outer_product(edge_feat, edge_grad)
    grad_dest = jax.ops.segment_sum(grad_pre_edge, edge_dst, row_count)
    grad_extended = jax.ops.segment_sum(
        jnp.concatenate([numer_edge * gating, grad_pre_edge], 1),
        edge_src,
        row_count + halo_send.shape[0],
    )
    returned = return_sources(grad_extended[row_count:])
    grad_source = grad_extended[:row_count].at[halo_send].add(returned)
    proj_grad = jnp.concatenate(
        [grad_message, grad_source[:, :model_width], grad_dest, grad_source[:, model_width:]], 1
    ).astype(jnp.bfloat16)
    grad_w_proj = outer_product(hidden_low, proj_grad)
    grad_hidden = (
        grad_mixed
        + grad_two
        + times_transposed(proj_grad, w_proj)
        + times_transposed(qkv_grad, w_qkv)
    )
    weight_grads = (grad_w_proj, grad_w_edge, grad_w_qkv, grad_w_out, grad_w_up, grad_w_down)
    return (
        grad_hidden,
        weight_grads,
        jnp.stack([gain_one, gain_two, gain_three]),
        jnp.stack([shift_one, shift_two, shift_three]),
    )


def per_device(
    node_input,
    edge_feat,
    graph_ids,
    edge_src,
    edge_dst,
    halo_send,
    w_proj,
    w_edge,
    w_qkv,
    w_out,
    w_up,
    w_down,
    norm_gain,
    norm_shift,
    cotangent,
):
    group_graphs = lax.all_gather(graph_ids, "nodes", axis=0, tiled=True)
    node_total = node_input.shape[0] * lax.axis_size("nodes") * lax.axis_size("rep")
    layer_count = w_proj.shape[0]
    layer_params = [
        (
            w_proj[layer_index],
            w_edge[layer_index],
            w_qkv[layer_index],
            w_out[layer_index],
            w_up[layer_index],
            w_down[layer_index],
            norm_gain[layer_index],
            norm_shift[layer_index],
        )
        for layer_index in range(layer_count)
    ]
    hidden = node_input.astype(jnp.float32)
    saved_all = []
    for layer_index in range(layer_count):
        hidden, saved = layer_forward(
            hidden,
            layer_params[layer_index],
            edge_feat,
            edge_src,
            edge_dst,
            halo_send,
            graph_ids,
            group_graphs,
            node_total,
        )
        saved_all.append(saved)
    grad_hidden = cotangent.astype(jnp.float32)
    weight_parts = [None] * layer_count
    gain_parts = [None] * layer_count
    shift_parts = [None] * layer_count
    for layer_index in range(layer_count - 1, -1, -1):
        (
            grad_hidden,
            weight_parts[layer_index],
            gain_parts[layer_index],
            shift_parts[layer_index],
        ) = layer_backward(
            grad_hidden,
            layer_params[layer_index],
            saved_all[layer_index],
            edge_feat,
            edge_src,
            edge_dst,
            halo_send,
            graph_ids,
            group_graphs,
            node_total,
        )
    proj_local = jnp.stack([weight_parts[layer_index][0] for layer_index in range(layer_count)])
    edge_local = jnp.stack([weight_parts[layer_index][1] for layer_index in range(layer_count)])
    qkv_local = jnp.stack([weight_parts[layer_index][2] for layer_index in range(layer_count)])
    out_local = jnp.stack([weight_parts[layer_index][3] for layer_index in range(layer_count)])
    up_local = jnp.stack([weight_parts[layer_index][4] for layer_index in range(layer_count)])
    down_local = jnp.stack([weight_parts[layer_index][5] for layer_index in range(layer_count)])
    grad_proj, grad_edge, grad_qkv, grad_out, grad_up, grad_down = lax.psum(
        (proj_local, edge_local, qkv_local, out_local, up_local, down_local), ("nodes", "rep")
    )
    return (
        hidden,
        grad_hidden,
        grad_proj,
        grad_edge,
        grad_qkv,
        grad_out,
        grad_up,
        grad_down,
        jnp.stack(gain_parts),
        jnp.stack(shift_parts),
    )


def solution(mesh):
    in_specs = (
        P(("rep", "nodes"), None),
        P(("rep", "nodes"), None),
        P(("rep", "nodes")),
        P(("rep", "nodes")),
        P(("rep", "nodes")),
        P(("rep", "nodes")),
        P(),
        P(),
        P(),
        P(),
        P(),
        P(),
        P(),
        P(),
        P(("rep", "nodes"), None),
    )
    out_specs = (
        P(("rep", "nodes"), None),
        P(("rep", "nodes"), None),
        P(),
        P(),
        P(),
        P(),
        P(),
        P(),
        P(),
        P(),
    )
    N, M = mesh.shape["nodes"], mesh.shape["rep"]
    fused = N in (4, 8) and M % 2 == 0 and 512 % (16 * N * M) == 0
    return jax.shard_map(
        functools.partial(fused_device, N, M) if fused else per_device,
        mesh=mesh, in_specs=in_specs, out_specs=out_specs, check_vma=False,
    )
```

```python
import functools
import math

import jax
import jax.numpy as jnp
from jax import lax
from jax.experimental import pallas as pl
from jax.experimental.pallas import tpu as pltpu
from jax.sharding import PartitionSpec as P

HEADS = 8
HEAD_DIM = 32
NEG = -1e30
NORM_EPS = 1e-05
GATE_EPS = 1e-06
F32, BF16, I32 = jnp.float32, jnp.bfloat16, jnp.int32
MESH = pl.DeviceIdType.MESH
SYNCS = 7
GROUPS = (
    ("early", 1, 0, 2560, ("core", "y", "nodes")),
    ("conv", 1, 0, 2560, ("core", "y", "nodes")),
    ("qkv", 1, 0, 1536, ("core", "y", "nodes")),
    ("early", 0, 0, 2560, ("core", "y", "nodes")),
    ("conv", 0, 0, 2560, ("core", "y", "nodes")),
    ("qkv", 0, 0, 1024, ("rep", "nodes")),
    ("qkv", 0, 1024, 512, ("nodes", "rep")),
)


def dot(left, right):
    return lax.dot_general(
        left, right, (((1,), (0,)), ((), ())), preferred_element_type=F32
    )


def dot_nt(left, right):
    return lax.dot_general(
        left, right, (((1,), (1,)), ((), ())), preferred_element_type=F32
    )


def dot_tn(left, right):
    return lax.dot_general(
        left, right, (((0,), (0,)), ((), ())), preferred_element_type=F32
    )


def split(value):
    high = value.astype(BF16)
    return high, (value - high.astype(F32)).astype(BF16)


def select_rows(onehot, value):
    high, low = split(value)
    return dot(onehot, high) + dot(onehot, low)


def sigmoid(value):
    return 1.0 / (1.0 + jnp.exp(-value))


def silu_slope(value):
    logistic = sigmoid(value)
    return logistic * (1.0 + value * (1.0 - logistic))


def col_sum(value):
    return jnp.sum(value, axis=0, keepdims=True)


def pack(first, second, third, fourth):
    halves = []
    for row in (first, second, third, fourth):
        halves += [row[:, :128], row[:, 128:]]
    return jnp.concatenate(halves, 0)


def unpack(tile):
    return [
        jnp.concatenate([tile[2 * i : 2 * i + 1], tile[2 * i + 1 : 2 * i + 2]], 1)
        for i in range(4)
    ]


def combine_pair(tiles, count):
    mean = jnp.mean(tiles[:, 0:4], 0)
    off = tiles[:, 0:4] - mean
    return jnp.concatenate([mean, jnp.sum(tiles[:, 4:8] + count * off * off, 0)], 0)


def combine_last(tiles, count):
    mean = jnp.mean(tiles[:, 0:2], 0)
    off = tiles[:, 0:2] - mean
    return jnp.concatenate(
        [
            mean,
            jnp.sum(tiles[:, 2:4], 0),
            jnp.sum(tiles[:, 4:6] + count * off * off, 0),
            jnp.sum(tiles[:, 6:8] + off * tiles[:, 2:4], 0),
        ],
        0,
    )


def combine_sum(tiles, count):
    return jnp.sum(tiles, 0)


class Refs:
    pass


def axis_sizes(N, M):
    return dict(core=2, y=M // 2, x=2, z=N // 2, rep=M, nodes=N)


def scratch_list(N, M, L, R, E):
    NZ, NB, G = N // 2, N // 4, N * R
    D, FF, W, HH = 256, 512, 4 * R, HEADS // 2 * R
    dma = lambda *shape: pltpu.SemaphoreType.DMA(shape)
    vm = lambda dtype, *shape: pltpu.VMEM(shape, dtype)
    names = dict(
        gb=vm(BF16, L, N, R, D),
        xs=vm(BF16, L, N, R, D),
        meta=vm(I32, N, 8, 256),
        ef=vm(BF16, E, D),
        cot=vm(BF16, R, D),
        wp=vm(BF16, L, D, 4 * D),
        we=vm(BF16, L, D, D),
        wqkv=vm(BF16, L, D, 3 * D),
        wo=vm(BF16, L, D, D),
        wu=vm(BF16, L, D, FF),
        wd=vm(BF16, L, FF, D),
        st1=vm(F32, SYNCS, M * N, 8, 128),
        gain=vm(F32, L, 8, D),
        shift=vm(F32, L, 8, D),
        ggain=vm(F32, L, 8, D),
        gshift=vm(F32, L, 8, D),
        iv=vm(F32, L, 8, D),
        moff=vm(F32, N, 8, D),
        move=vm(F32, 8, D),
        T=vm(BF16, E, R),
        TT=vm(BF16, R, E),
        S=vm(BF16, E, 256),
        ST=vm(BF16, 256, E),
        efT=vm(BF16, D, E),
        HP=vm(BF16, 32, R),
        HN=vm(BF16, 32, R),
        A=vm(BF16, R, 64),
        bias=vm(F32, R, G),
        ce=vm(F32, L, E, D),
        xf=vm(F32, L + 1, R, D),
        xe=vm(BF16, L, 256, D),
        xeT=vm(BF16, D, 256),
        gate=vm(F32, L, E, D),
        bs=vm(BF16, L, E, D),
        num=vm(F32, L, R, D),
        den=vm(F32, L, R, D),
        z0=vm(F32, L, R, D),
        z1=vm(F32, L, R, D),
        z2=vm(F32, L, R, D),
        kk=vm(BF16, L, G, D),
        vv=vm(BF16, L, G, D),
        kT=vm(BF16, D, G),
        vT=vm(BF16, D, G),
        od=vm(F32, NB, R, D),
        md=vm(F32, NB, R, D),
        ld=vm(F32, NB, R, D),
        rb=vm(F32, L, NB, R, D),
        pst=vm(BF16, L, HEADS * R, G),
        oraw=vm(F32, L, R, D),
        ob=vm(BF16, L, R, D),
        mb=vm(BF16, L, R, D),
        u=vm(F32, L, R, FF),
        g=vm(BF16, L, R, FF),
        dy=vm(F32, R, D),
        dmix=vm(F32, R, D),
        dxo=vm(F32, R, D),
        dob=vm(F32, R, D),
        dq=vm(F32, R, D),
        qm=vm(BF16, L, 2, HH, 128),
        qmT=vm(BF16, 2, 128, HH),
        dom=vm(BF16, HH, 128),
        dss=vm(BF16, HH, W),
        dkv=vm(BF16, 2 * D, W),
        gkv=vm(F32, 2 * D, D),
        dce=vm(BF16, E, D),
        dproj=vm(BF16, 4, 256, D),
        dxs=vm(BF16, L, NZ, 2, R, D),
        rs1=vm(BF16, L, NZ, R, D),
        cs=vm(BF16, L, NZ, R, D),
        rs2=vm(BF16, L, NZ, R, D),
        ro=vm(BF16, L, 3, R, D),
        hs=vm(BF16, L, 2, 32, D),
        hr=vm(BF16, L, 2, 32, D),
    )
    names.update(
        gs_early=vm(BF16, L, 2560, 128),
        gs_conv=vm(BF16, L, 2560, 128),
        gs_qkv=vm(BF16, L, 1536, 128),
    )
    sizes = axis_sizes(N, M)
    for g, (_, _, _, rows, stages) in enumerate(GROUPS):
        names[f"go{g}"] = vm(BF16, rows, 128)
        left = rows
        for k, axis in enumerate(stages):
            left //= sizes[axis]
            names[f"ga{g}_{k}"] = vm(BF16, sizes[axis] - 1, left, 128)
            if k < len(stages) - 1:
                names[f"gh{g}_{k}"] = vm(BF16, left, 128)
    names.update(
        ar_s=dma(len(GROUPS), 8),
        ar_r=dma(len(GROUPS), 8),
        ar_l=dma(len(GROUPS)),
        load=dma(10),
        store=dma(2),
        meta_s=dma(1),
        meta_r=dma(1),
        st1_s=dma(SYNCS),
        st1_r=dma(SYNCS),
        agc_s=dma(L, NZ),
        agc_r=dma(L, NZ),
        agp_s=dma(L, NZ),
        agp_r=dma(L, NZ),
        rsp_s=dma(L, NZ),
        rsp_r=dma(L, NZ),
        ro_s=dma(L, 3),
        ro_r=dma(L, 3),
        rsc_s=dma(L, NZ),
        rsc_r=dma(L, NZ),
        hal_s=dma(L, 2),
        hal_r=dma(L, 2),
    )
    return names


IN_NAMES = (
    "x_in", "ids", "edge_src", "edge_dst", "halo", "ef_h", "wp_h", "we_h", "wqkv_h", "wo_h", "wu_h", "wd_h",
    "gain_in", "shift_in", "cot_h",
)
OUT_NAMES = ("out_act", "grad_in", *(f"gout{g}" for g in range(len(GROUPS))), "ggain_out", "gshift_out")


def kernel(N, M, L, names, *args):
    r_ = Refs()
    for name, ref in zip(IN_NAMES + OUT_NAMES + tuple(names), args, strict=True):
        setattr(r_, name, ref)
    R, D = r_.x_in.shape
    E = r_.ef.shape[0]
    NZ, NB, G, W = N // 2, N // 4, N * R, 4 * R
    HK = HEADS // 2
    total = float(N * M * R)
    scale = HEAD_DIM ** -0.5
    me = lax.axis_index("nodes")
    rep = lax.axis_index("rep")
    z = me // 2
    par = me % 2
    partner = 2 * z + (1 - par)
    prev = (me + N - 1) % N
    nxt = (me + 1) % N
    zh, zl = z // 2, z % 2
    z_to = lambda t: 2 * ((zh + t // 2) % NB) + (zl + t % 2) % 2
    z_from = lambda t: 2 * ((zh + NB - t // 2) % NB) + (zl + t % 2) % 2

    def remote(src, dst, s_sem, r_sem, **where):
        return pltpu.make_async_remote_copy(
            src_ref=src, dst_ref=dst, send_sem=s_sem, recv_sem=r_sem,
            device_id=where, device_id_type=MESH,
        )

    def send(src, dst, s_sem, r_sem, **where):
        remote(src, dst, s_sem, r_sem, **where).start()

    def send_rows(src, dst, rows, s_sem, r_sem, **where):
        pieces = next(p for p in range(1, rows) if rows % (16 * p) == 0 and rows // p <= 128)
        for at in range(0, rows, rows // pieces):
            cut = pl.ds(at, rows // pieces)
            send(src.at[cut], dst.at[cut], s_sem, r_sem, **where)

    def arrive(dst, r_sem):
        remote(dst, dst, r_sem, r_sem, nodes=partner).wait_recv()

    def sent(src, s_sem):
        remote(src, src, s_sem, s_sem, nodes=partner).wait_send()

    def when(condition, *acts):
        @pl.when(condition)
        def _():
            for act in acts:
                act()

    loads = [
        pltpu.make_async_copy(getattr(r_, f"{name}_h"), getattr(r_, name), r_.load.at[i])
        for i, name in enumerate(("ef", "we", "wqkv", "wp", "wo", "wu", "wd", "cot"))
    ]
    own_rows = pltpu.make_async_copy(r_.x_in, r_.gb.at[0, me], r_.load.at[8])
    own_rows.start()
    for load in loads:
        load.start()

    barrier = pltpu.get_barrier_semaphore()
    for dr in range(M):
        for d in range(N):
            if dr + d > 0:
                pl.semaphore_signal(barrier, inc=1, device_id={"rep": (rep + dr) % M, "nodes": (me + d) % N},
                                    device_id_type=MESH)
    pl.semaphore_wait(barrier, M * N - 1)

    def gather_start(l):
        mine = r_.gb.at[l, me]
        send_rows(mine, mine, R, r_.agp_s.at[l, 0], r_.agp_r.at[l, 0], nodes=partner)
        send_rows(mine, mine, R, r_.agc_s.at[l, 1], r_.agc_r.at[l, 1], nodes=2 * z_to(1) + par)
        send_rows(mine, mine, R, r_.agp_s.at[l, 1], r_.agp_r.at[l, 1], nodes=2 * z_to(1) + 1 - par)
        for t in range(2, NZ):
            send_rows(mine, mine, R, r_.agc_s.at[l, t], r_.agc_r.at[l, t], nodes=2 * z_to(t) + par)

    def gather_pass(l, t):
        piece = r_.gb.at[l, 2 * z_from(t) + par]
        arrive(piece, r_.agc_r.at[l, t])
        send_rows(piece, piece, R, r_.agp_s.at[l, t], r_.agp_r.at[l, t], nodes=partner)

    def gather_take(l, t):
        arrive(r_.gb.at[l, 2 * z_from(t) + 1 - par], r_.agp_r.at[l, t])

    def sync_start(k, tile):
        mine = rep * N + me
        r_.st1[k, mine] = tile
        for dr in range(M):
            for d in range(N):
                if dr + d > 0:
                    send(r_.st1.at[k, mine], r_.st1.at[k, mine], r_.st1_s.at[k], r_.st1_r.at[k],
                         rep=(rep + dr) % M, nodes=(me + d) % N)

    def sync_finish(k, combine):
        arrive(r_.st1.at[k, 0 : M * N - 1], r_.st1_r.at[k])
        return unpack(combine(r_.st1[k], float(R)))

    sizes = axis_sizes(N, M)
    core, row = rep % 2, rep // 2
    places = dict(
        core=(core, lambda t: dict(rep=2 * row + t)),
        y=(row, lambda t: dict(rep=2 * t + core)),
        x=(par, lambda t: dict(nodes=2 * z + t)),
        z=(z, lambda t: dict(nodes=2 * t + par)),
        rep=(rep, lambda t: dict(rep=t)),
        nodes=(me, lambda t: dict(nodes=t)),
    )

    def reduce_step(g, step):
        name, layer, first, rows, stages = GROUPS[g]
        K = len(stages)
        gs, out = getattr(r_, f"gs_{name}").at[layer, first : first + rows], getattr(r_, f"go{g}")
        count, offset = [rows], [0]
        for axis in stages:
            count.append(count[-1] // sizes[axis])
            offset.append(offset[-1] + places[axis][0] * count[-1])
        take = lambda start, size: pl.ds(pl.multiple_of(start, 16), size)
        if 1 <= step <= K:
            k = step - 1
            got = getattr(r_, f"ga{g}_{k}")
            arrive(got, r_.ar_r.at[g, k])
            held = gs if k == 0 else getattr(r_, f"gh{g}_{k - 1}")
            index = places[stages[k]][0]
            acc = held[take(index * count[k + 1], count[k + 1])].astype(F32)
            for slot in range(sizes[stages[k]] - 1):
                acc = acc + got[slot].astype(F32)
            if step < K:
                getattr(r_, f"gh{g}_{k}")[...] = acc.astype(BF16)
            else:
                out[take(offset[K], count[K])] = acc.astype(BF16)
        elif step > K:
            k = 2 * K - step
            arrive(out.at[0 : (sizes[stages[k]] - 1) * count[k + 1]], r_.ar_r.at[g, step - 1])
        if step < K:
            held = gs if step == 0 else getattr(r_, f"gh{g}_{step - 1}")
            index, device = places[stages[step]]
            size = sizes[stages[step]]
            for d in range(1, size):
                to = (index + d) % size
                send_rows(held.at[take(to * count[step + 1], count[step + 1])], getattr(r_, f"ga{g}_{step}").at[d - 1],
                     count[step + 1], r_.ar_s.at[g, step], r_.ar_r.at[g, step], **device(to))
        elif step < 2 * K:
            k = 2 * K - 1 - step
            index, device = places[stages[k]]
            size = sizes[stages[k]]
            here = out.at[take(offset[k + 1], count[k + 1])]
            for d in range(1, size):
                send_rows(here, here, count[k + 1], r_.ar_s.at[g, step], r_.ar_r.at[g, step],
                          **device((index + d) % size))
        else:
            pltpu.make_async_copy(out, getattr(r_, f"gout{g}"), r_.ar_l.at[g]).start()

    def reduce_drain(g):
        _, _, _, rows, stages = GROUPS[g]
        K, left = len(stages), rows
        out = getattr(r_, f"go{g}")
        for k, axis in enumerate(stages):
            left //= sizes[axis]
            for step in (k, 2 * K - 1 - k):
                sent(out.at[0 : (sizes[axis] - 1) * left], r_.ar_s.at[g, step])
        pltpu.make_async_copy(out, getattr(r_, f"gout{g}"), r_.ar_l.at[g]).wait()

    def put(buf, l, at, value):
        rows = value.shape[0]
        for c in range(value.shape[1] // 128):
            buf[l, at : at + rows] = value[:, 128 * c : 128 * (c + 1)].astype(BF16)
            at += rows
        return at

    lane_head = lax.broadcasted_iota(I32, (R, 128), 1) // HEAD_DIM

    def by_head(parts):
        out = parts[0]
        for k in range(1, HK):
            out = jnp.where(lane_head == k, parts[k], out)
        return out

    r_.meta[me] = jnp.full((8, 256), -1, I32)
    r_.meta[me, 0:1, 0:R] = r_.ids[...].reshape(1, R)
    r_.meta[me, 1:2, 0:48] = r_.halo[...].reshape(1, 48)
    for d in range(1, N):
        send(r_.meta.at[me], r_.meta.at[me], r_.meta_s.at[0], r_.meta_r.at[0], nodes=(me + d) % N)
    own_rows.wait()
    gather_start(0)

    src_row = r_.edge_src[...].reshape(1, E)
    src_row = jnp.where(src_row < R + 24, src_row, src_row + 8)
    dst_row = r_.edge_dst[...].reshape(1, E)
    src_col = jnp.broadcast_to(src_row, (128, E)).T[:, 0:1]
    dst_col = jnp.broadcast_to(dst_row, (128, E)).T[:, 0:1]
    as_mask = lambda cond: cond.astype(F32).astype(BF16)
    r_.T[...] = as_mask(dst_col == lax.broadcasted_iota(I32, (E, R), 1))
    r_.TT[...] = as_mask(dst_row == lax.broadcasted_iota(I32, (R, E), 0))
    r_.S[...] = as_mask(src_col == lax.broadcasted_iota(I32, (E, 256), 1))
    r_.ST[...] = as_mask(src_row == lax.broadcasted_iota(I32, (256, E), 0))
    loads[0].wait()
    r_.efT[...] = r_.ef[...].T
    loads[1].wait()
    for l in range(L):
        r_.ce[l] = dot(r_.ef[...], r_.we[l])
        for k in range(3):
            r_.gain[l, k : k + 1] = r_.gain_in[k, l : l + 1]
            r_.shift[l, k : k + 1] = r_.shift_in[k, l : l + 1]
    r_.xf[0] = r_.gb[0, me].astype(F32)
    r_.moff[...] = jnp.zeros((N, 8, D), F32)
    r_.move[0:1] = jnp.ones((1, D), F32)
    r_.move[1:2] = jnp.zeros((1, D), F32)
    for load in loads[2:]:
        load.wait()

    arrive(r_.meta.at[0 : N - 1], r_.meta_r.at[0])
    id_col = jnp.broadcast_to(r_.meta[me][0:1, 0:R], (128, R)).T[:, 0:1]
    id_row = jnp.concatenate([r_.meta[j][0:1, 0:R] for j in range(N)], 1)
    r_.bias[...] = jnp.where(id_col == id_row, 0.0, NEG)

    def halo_onehot(device, start):
        col = jnp.broadcast_to(r_.meta[device][1:2, 0:128], (128, 128)).T[start : start + 24, 0:1]
        hot = (col == lax.broadcasted_iota(I32, (24, R), 1)).astype(F32)
        return jnp.concatenate([hot, jnp.zeros((8, R), F32)], 0).astype(BF16)

    r_.HP[...] = halo_onehot(prev, 24)
    r_.HN[...] = halo_onehot(nxt, 0)
    r_.A[...] = as_mask(r_.meta[me][1:2, 0:64] == lax.broadcasted_iota(I32, (R, 64), 0))

    factor_exp = scale * math.log2(math.e)

    def prepare_queries(l):
        q = dot(r_.xs[l, me], r_.wqkv[l, :, :D]).astype(BF16).astype(F32)
        for hf in range(2):
            for k in range(HK):
                part = jnp.where(lane_head == k, q[:, 128 * hf : 128 * (hf + 1)], 0.0)
                r_.qm[l, hf, k * R : (k + 1) * R] = part.astype(BF16)

    def head_rows(hf, k, count=1):
        return pl.ds(pl.multiple_of((hf * HK + k) * R, 64), count * R)

    def lane_half(hf):
        return pl.ds(pl.multiple_of(hf * 128, 128), 128)

    def attention_block(l, i, middle):
        half = (zh + NB - i) % NB
        rows = pl.ds(pl.multiple_of(half * W, 128), W)
        x = r_.xs[l, pl.ds(4 * half, 4)].reshape(W, D)
        key = dot(x, r_.wqkv[l, :, D : 2 * D]).astype(BF16)
        r_.kk[l, rows] = key
        r_.kT[:, rows] = key.T
        r_.vv[l, rows] = dot(x, r_.wqkv[l, :, 2 * D :]).astype(BF16)

        def heads(hf, carry):
            lanes = lane_half(hf)
            tops, sums, outs = [], [], []
            for c in range(HK // 2):
                scores = dot(r_.qm[l, hf, 2 * c * R : 2 * (c + 1) * R], r_.kT[lanes, rows])
                for k in range(2):
                    s = scores[k * R : (k + 1) * R] + r_.bias[:, rows]
                    top = jnp.max(s, 1, keepdims=True)
                    e = jnp.exp2((s - top) * factor_exp)
                    tops.append(top)
                    sums.append(jnp.sum(e, 1, keepdims=True))
                    r_.pst[l, head_rows(hf, 2 * c + k), rows] = e.astype(BF16)
                o = dot(r_.pst[l, head_rows(hf, 2 * c, 2), rows], r_.vv[l, rows, lanes])
                outs += [o[0:R], o[R : 2 * R]]
            r_.md[i, :, lanes] = by_head([jnp.broadcast_to(v, (R, 128)) for v in tops])
            r_.ld[i, :, lanes] = by_head([jnp.broadcast_to(v, (R, 128)) for v in sums])
            r_.od[i, :, lanes] = by_head(outs)
            middle(i, hf)
            return carry

        lax.fori_loop(0, 2, heads, 0)

    def attention_end(l):
        top = r_.md[0]
        for i in range(1, NB):
            top = jnp.maximum(top, r_.md[i])
        factors = [jnp.exp2((r_.md[i] - top) * factor_exp) for i in range(NB)]
        inv = 1.0 / sum(factors[i] * r_.ld[i] for i in range(NB))
        o = jnp.zeros((R, D), F32)
        for i in range(NB):
            r_.rb[l, i] = factors[i] * inv
            o = o + factors[i] * inv * r_.od[i]
        r_.oraw[l] = o
        ob = o.astype(BF16)
        r_.ob[l] = ob
        t1 = r_.xf[l] + dot(ob, r_.wo[l])
        r_.z1[l] = t1
        mean1 = col_sum(t1) / R
        return mean1, col_sum((t1 - mean1) * (t1 - mean1))

    def convolution(l):
        xs = r_.xs
        xb = xs[l, me]
        r_.xe[l, 0:R] = xb
        r_.xe[l, R : R + 32] = dot(r_.HP[...], xs[l, prev]).astype(BF16)
        r_.xe[l, R + 32 : R + 64] = dot(r_.HN[...], xs[l, nxt]).astype(BF16)
        xe = r_.xe[l]
        tab_b = dot(xe, r_.wp[l, :, D : 2 * D]).astype(BF16)
        tab_e = dot(xe, r_.wp[l, :, 3 * D :]).astype(BF16)
        pa = dot(xb, r_.wp[l, :, 0:D])
        pd = dot(xb, r_.wp[l, :, 2 * D : 3 * D])
        bs = dot(r_.S[...], tab_b)
        r_.bs[l] = bs.astype(BF16)
        gate = sigmoid(select_rows(r_.T[...], pd) + dot(r_.S[...], tab_e) + r_.ce[l])
        r_.gate[l] = gate
        num = select_rows(r_.TT[...], gate * bs)
        den = select_rows(r_.TT[...], gate)
        r_.num[l] = num
        r_.den[l] = den
        msg = pa + num / (den + GATE_EPS)
        r_.z0[l] = msg

    def forward(l, carry):
        def ready(js):
            for j in js:
                moved = (r_.gb[l, j].astype(F32) + r_.moff[j, 0:1]) * r_.move[0:1] + r_.move[1:2]
                r_.xs[l, j] = moved.astype(BF16)

        r_.xs[l, me] = r_.xf[l].astype(BF16)
        prepare_queries(l)
        arrive(r_.gb.at[l, 2 * z_from(1) + par], r_.agc_r.at[l, 1])
        gather_take(l, 0)
        gather_take(l, 1)
        ready([partner, 2 * z_from(1) + par, 2 * z_from(1) + 1 - par])

        def middle(i, hf):
            when((i == 0) & (hf == 0), *[functools.partial(gather_pass, l, t) for t in range(2, NZ)])

        def block(i, carry):
            attention_block(l, i, middle)

            @pl.when(i == 0)
            def _():
                for t in range(2, NZ):
                    gather_take(l, t)
                ready([2 * z_from(t) + p for t in range(2, NZ) for p in range(2)])
                convolution(l)

            return carry

        lax.fori_loop(0, NB, block, 0)
        mean1, sq1 = attention_end(l)
        msg = r_.z0[l]
        mean0 = col_sum(msg) / R
        sq0 = col_sum((msg - mean0) * (msg - mean0))
        sync_start(2 * l, pack(mean0, mean1, sq0, sq1))
        mean0, mean1, sq0, sq1 = sync_finish(2 * l, combine_pair)
        inv0 = lax.rsqrt(sq0 / total + NORM_EPS)
        inv1 = lax.rsqrt(sq1 / total + NORM_EPS)
        r_.iv[l, 0:1] = inv0
        r_.iv[l, 1:2] = inv1
        z0 = (r_.z0[l] - mean0) * inv0
        z1 = (r_.z1[l] - mean1) * inv1
        r_.z0[l] = z0
        r_.z1[l] = z1
        n0 = z0 * r_.gain[l, 0:1] + r_.shift[l, 0:1]
        mix = r_.xf[l] + n0 * sigmoid(n0) + z1 * r_.gain[l, 1:2] + r_.shift[l, 1:2]
        mb = mix.astype(BF16)
        r_.mb[l] = mb
        u = dot(mb, r_.wu[l])
        r_.u[l] = u
        g = (u * sigmoid(u)).astype(BF16)
        r_.g[l] = g
        y = mix + dot(g, r_.wd[l])
        r_.z2[l] = y
        mean = col_sum(y) / R
        cent = y - mean
        k = 2 * l + 1
        dy = r_.cot[...].astype(F32)
        sync_start(k, pack(mean, col_sum(dy), col_sum(cent * cent), col_sum(dy * cent)))

        @pl.when(l < L - 1)
        def _():
            r_.gb[l + 1, me] = cent.astype(BF16)
            gather_start(l + 1)

        tot_mean, dy_sum, tot_sq, dy_cent = sync_finish(k, combine_last)
        inv2 = lax.rsqrt(tot_sq / total + NORM_EPS)
        r_.iv[l, 2:3] = inv2
        z2 = (r_.z2[l] - tot_mean) * inv2
        r_.z2[l] = z2
        gain, shift = r_.gain[l, 2:3], r_.shift[l, 2:3]
        r_.xf[l + 1] = z2 * gain + shift
        r_.gshift[l, 2:3] = dy_sum
        r_.ggain[l, 2:3] = dy_cent * inv2
        for j in range(N):
            tile = r_.st1[k, rep * N + j]
            r_.moff[j, 0:1] = jnp.concatenate([tile[0:1], tile[1:2]], 1) - tot_mean
        r_.move[0:1] = inv2 * gain
        r_.move[1:2] = shift
        return carry

    lax.fori_loop(0, L, forward, 0)
    act_copy = pltpu.make_async_copy(r_.xf.at[L], r_.out_act, r_.store.at[0])
    act_copy.start()

    def back_feed_forward(l, k):
        s2, g2 = r_.gshift[l, 2:3], r_.ggain[l, 2:3]
        d3 = r_.gain[l, 2:3] * r_.iv[l, 2:3] * (r_.dy[...] - s2 / total - r_.z2[l] * (g2 / total))
        db = d3.astype(BF16)
        dub = (dot_nt(db, r_.wd[l]) * silu_slope(r_.u[l])).astype(BF16)
        dmix = d3 + dot_nt(dub, r_.wu[l])
        r_.dmix[...] = dmix
        n0 = r_.z0[l] * r_.gain[l, 0:1] + r_.shift[l, 0:1]
        gy0 = dmix * silu_slope(n0)
        sync_start(k, pack(col_sum(dmix), col_sum(dmix * r_.z1[l]), col_sum(gy0), col_sum(gy0 * r_.z0[l])))
        at = put(r_.gs_early, l, 512, dot_tn(r_.mb[l], dub))
        put(r_.gs_early, l, at, dot_tn(r_.g[l], db))
        r_.vT[...] = r_.vv[l].T
        r_.xeT[...] = r_.xe[l].T
        for hf in range(2):
            r_.qmT[hf] = r_.qm[l, hf].T

    def back_norms(l, k):
        s1, g1, s0, g0 = sync_finish(k, combine_sum)
        r_.gshift[l, 1:2] = s1
        r_.ggain[l, 1:2] = g1
        r_.gshift[l, 0:1] = s0
        r_.ggain[l, 0:1] = g0
        dmix = r_.dmix[...]
        d2 = r_.gain[l, 1:2] * r_.iv[l, 1:2] * (dmix - s1 / total - r_.z1[l] * (g1 / total))
        dab = d2.astype(BF16)
        r_.dxo[...] = dmix + d2
        r_.dob[...] = dot_nt(dab, r_.wo[l]).astype(BF16).astype(F32)
        put(r_.gs_early, l, 0, dot_tn(r_.ob[l], dab))
        r_.gkv[...] = jnp.zeros((2 * D, D), F32)
        r_.dq[...] = jnp.zeros((R, D), F32)

    def back_attention_block(l, i, between):
        t1 = (i + 1) % NB
        half = (zh + t1) % NB
        rows = pl.ds(pl.multiple_of(half * W, 128), W)

        def heads(hf, carry):
            lanes = lane_half(hf)
            dos = r_.dob[:, lanes] * r_.rb[l, (NB - t1) % NB, :, lanes]
            prod = dos * r_.oraw[l, :, lanes]
            for k in range(HK):
                r_.dom[k * R : (k + 1) * R] = jnp.where(lane_head == k, dos, 0.0).astype(BF16)
            parts = []
            for c in range(HK // 2):
                both = slice(2 * c * R, 2 * (c + 1) * R)
                dp = dot(r_.dom[both], r_.vT[lanes, rows])
                for k in range(2):
                    h = 2 * c + k
                    delta = jnp.sum(jnp.where(lane_head == h, prod, 0.0), 1, keepdims=True)
                    ds = r_.pst[l, head_rows(hf, h), rows].astype(F32) * (dp[k * R : (k + 1) * R] - delta)
                    r_.dss[h * R : (h + 1) * R] = ds.astype(BF16)
                part = dot(r_.dss[both], r_.kk[l, rows, lanes])
                parts += [part[0:R], part[R : 2 * R]]
            r_.dq[:, lanes] += by_head(parts)
            dk = dot(r_.qmT[hf], r_.dss[...]) * scale
            r_.dkv[pl.ds(pl.multiple_of(hf * 128, 128), 128)] = dk.astype(BF16)
            dv = dot(r_.dom[...].T, r_.pst[l, head_rows(hf, 0, HK), rows])
            r_.dkv[pl.ds(pl.multiple_of(D + hf * 128, 128), 128)] = dv.astype(BF16)
            between(i, hf)
            return carry

        lax.fori_loop(0, 2, heads, 0)
        dx = dot(r_.wqkv[l, :, D:], r_.dkv[...]).T
        r_.dxs[l, pl.ds(2 * half, 2)] = dx.astype(BF16).reshape(2, 2, R, D)

        @pl.when(i < NB - 1)
        def _():
            for low in range(2):
                zb = 2 * half + low
                send_rows(r_.dxs.at[l, zb, 1 - par], r_.rs1.at[l, zb], R,
                     r_.rsp_s.at[l, 2 * i + low], r_.rsp_r.at[l, 2 * i + low], nodes=partner)

        @pl.when(i == NB - 1)
        def _():
            near = z_to(1)
            send_rows(r_.dxs.at[l, z, 1 - par], r_.ro.at[l, 0], R, r_.ro_s.at[l, 0], r_.ro_r.at[l, 0], nodes=partner)
            send_rows(r_.dxs.at[l, near, par], r_.ro.at[l, 1], R, r_.ro_s.at[l, 1], r_.ro_r.at[l, 1], nodes=2 * near + par)
            send_rows(r_.dxs.at[l, near, 1 - par], r_.ro.at[l, 2], R, r_.ro_s.at[l, 2], r_.ro_r.at[l, 2],
                 nodes=2 * near + 1 - par)

        r_.gkv[...] += dot(r_.dkv[...], r_.xs[l, pl.ds(4 * half, 4)].reshape(W, D))

    def pass_on(l, i, t):
        zb = z_to(t)
        arrive(r_.rs1.at[l, zb], r_.rsp_r.at[l, 2 * i + zb % 2])
        both = r_.dxs[l, zb, par].astype(F32) + r_.rs1[l, zb].astype(F32)
        r_.cs[l, zb] = both.astype(BF16)
        send_rows(r_.cs.at[l, zb], r_.rs2.at[l, z], R, r_.rsc_s.at[l, t], r_.rsc_r.at[l, t], nodes=2 * zb + par)

    def back_convolution(l):
        s0, g0 = r_.gshift[l, 0:1], r_.ggain[l, 0:1]
        inv_den = 1.0 / (r_.den[l] + GATE_EPS)
        n0 = r_.z0[l] * r_.gain[l, 0:1] + r_.shift[l, 0:1]
        gy0 = r_.dmix[...] * silu_slope(n0)
        dm = r_.gain[l, 0:1] * r_.iv[l, 0:1] * (gy0 - s0 / total - r_.z0[l] * (g0 / total))
        dnum = dm * inv_den
        dden = -dnum * r_.num[l] * inv_den
        dnum_e = select_rows(r_.T[...], dnum)
        dden_e = select_rows(r_.T[...], dden)
        gate = r_.gate[l]
        dgp = (dnum_e * r_.bs[l].astype(F32) + dden_e) * gate * (1.0 - gate)
        r_.dce[...] = dgp.astype(BF16)
        dpb = select_rows(r_.ST[...], dnum_e * gate).astype(BF16)
        dpe = select_rows(r_.ST[...], dgp).astype(BF16)
        dpd = select_rows(r_.TT[...], dgp).astype(BF16)
        dmb = dm.astype(BF16)
        dxe = dot_nt(dpb, r_.wp[l, :, D : 2 * D]) + dot_nt(dpe, r_.wp[l, :, 3 * D :])
        r_.hs[l, 0] = dxe[R : R + 32].astype(BF16)
        r_.hs[l, 1] = dxe[R + 32 : R + 64].astype(BF16)
        send(r_.hs.at[l, 0], r_.hr.at[l, 1], r_.hal_s.at[l, 0], r_.hal_r.at[l, 0], nodes=prev)
        send(r_.hs.at[l, 1], r_.hr.at[l, 0], r_.hal_s.at[l, 1], r_.hal_r.at[l, 1], nodes=nxt)
        r_.dxo[...] += (
            dxe[0:R]
            + dot_nt(dmb, r_.wp[l, :, 0:D])
            + dot_nt(dpd, r_.wp[l, :, 2 * D : 3 * D])
        )
        r_.dproj[0, 0:R] = dmb
        r_.dproj[1] = dpb
        r_.dproj[2, 0:R] = dpd
        r_.dproj[3] = dpe

    def conv_weight_grads(l):
        at = 0
        for c in range(4):
            width = R if c % 2 == 0 else 256
            at = put(r_.gs_conv, l, at, dot(r_.xeT[:, 0:width], r_.dproj[c, 0:width]))
        put(r_.gs_conv, l, at, dot(r_.efT[...], r_.dce[...]))

    def back_input(l):
        dx = r_.dxo[...]
        dx = dx + r_.dxs[l, z, par].astype(F32)
        for slot in range(3):
            arrive(r_.ro.at[l, slot], r_.ro_r.at[l, slot])
            dx = dx + r_.ro[l, slot].astype(F32)
        for t in range(2, NZ):
            c = z_from(t)
            arrive(r_.rs2.at[l, c], r_.rsc_r.at[l, t])
            dx = dx + r_.rs2[l, c].astype(F32)
        arrive(r_.hr.at[l, 0], r_.hal_r.at[l, 1])
        arrive(r_.hr.at[l, 1], r_.hal_r.at[l, 0])
        back = jnp.concatenate(
            [r_.hr[l, 0].astype(F32)[0:24], r_.hr[l, 1].astype(F32)[0:24], jnp.zeros((16, D), F32)], 0
        )
        return dx + dot(r_.A[...], back.astype(BF16))

    r_.dy[...] = r_.cot[...].astype(F32)

    E1, C1, Q1, E0, C0, QK0, V0 = range(len(GROUPS))

    def steps(*pairs):
        return [functools.partial(reduce_step, g, k) for g, k in pairs]

    def backward(b, carry):
        l = L - 1 - b
        first, last = b == 0, b == L - 1
        k = 4 + 2 * b
        back_feed_forward(l, k)
        when(last, *steps((C1, 4), (Q1, 1), (E1, 5)))
        back_norms(l, k)
        when(first, *steps((E1, 0)))
        when(last, *steps((E0, 0), (Q1, 2), (E1, 6), (C1, 5)))
        back_convolution(l)
        conv_weight_grads(l)
        when(first, *steps((E1, 1), (C1, 0)))
        when(last, *steps((E0, 1), (C0, 0), (Q1, 3), (C1, 6)))

        def between(i, hf):
            when(first & (i == 0) & (hf == 0), *steps((C1, 1)))
            when(first & (i == 0) & (hf == 1), *steps((E1, 2)))
            when(first & (i == 1) & (hf == 0), *steps((C1, 2)))
            when(first & (i == 1) & (hf == 1), *steps((E1, 3)))
            when(last & (i == 0) & (hf == 0), *steps((C0, 1)))
            when(last & (i == 0) & (hf == 1), *steps((E0, 2), (Q1, 4)))
            when(last & (i == 1) & (hf == 0), *steps((C0, 2)))
            when(last & (i == 1) & (hf == 1), *steps((E0, 3), (Q1, 5)))
            for t in range(2, NZ):
                when((i == 1) & (hf == 0), functools.partial(pass_on, l, 0, t))

        def block(i, carry):
            back_attention_block(l, i, between)
            return carry

        lax.fori_loop(0, NB, block, 0)
        dqb = (r_.dq[...] * scale).astype(BF16)
        r_.dxo[...] += dot_nt(dqb, r_.wqkv[l, :, 0:D])
        at = put(r_.gs_qkv, l, 0, dot(r_.xeT[:, 0:R], dqb))
        put(r_.gs_qkv, l, at, r_.gkv[...].T)
        when(first, *steps((Q1, 0)))

        @pl.when(first)
        def _():
            dx = back_input(l)
            r_.dy[...] = dx
            below = L - 2
            zero_row = jnp.zeros((1, D), F32)
            sync_start(5, pack(col_sum(dx), col_sum(dx * r_.z2[below]), zero_row, zero_row))
            for step in steps((C1, 3), (E1, 4)):
                step()
            s2, g2, _, _ = sync_finish(5, combine_sum)
            r_.gshift[below, 2:3] = s2
            r_.ggain[below, 2:3] = g2

        return carry

    lax.fori_loop(0, L, backward, 0)
    for step in steps((QK0, 0), (V0, 0), (C0, 3), (E0, 4), (Q1, 6), (V0, 1), (QK0, 1)):
        step()
    r_.dy[...] = back_input(0)
    in_copy = pltpu.make_async_copy(r_.dy, r_.grad_in, r_.store.at[1])
    in_copy.start()
    for step in steps(
        (C0, 4), (E0, 5), (V0, 2), (QK0, 2),
        (C0, 5), (E0, 6), (V0, 3), (QK0, 3),
        (C0, 6), (V0, 4), (QK0, 4),
    ):
        step()
    for l in range(L):
        for k in range(3):
            r_.ggain_out[k, l : l + 1] = r_.ggain[l, k : k + 1]
            r_.gshift_out[k, l : l + 1] = r_.gshift[l, k : k + 1]
    for g in range(len(GROUPS)):
        reduce_drain(g)
    sent(r_.meta.at[0 : N - 1], r_.meta_s.at[0])
    for k in range(SYNCS):
        sent(r_.st1.at[k, 0 : M * N - 1], r_.st1_s.at[k])
    for l in range(L):
        for t in range(NZ):
            sent(r_.gb.at[l, 0], r_.agp_s.at[l, t])
            if t > 0:
                sent(r_.gb.at[l, 0], r_.agc_s.at[l, t])
            if t > 1:
                sent(r_.rs1.at[l, 0], r_.rsc_s.at[l, t])
        for slot in range(2 * (NB - 1)):
            sent(r_.rs1.at[l, 0], r_.rsp_s.at[l, slot])
        for slot in range(3):
            sent(r_.ro.at[l, 0], r_.ro_s.at[l, slot])
        for side in range(2):
            sent(r_.hs.at[l, 0], r_.hal_s.at[l, side])
    act_copy.wait()
    in_copy.wait()


def finish_kernel(act_h, gin_h, *refs):
    n = len(GROUPS)
    held, (ggain_h, gshift_h), refs = refs[:n], refs[n : n + 2], refs[n + 2 :]
    act_o, gin_o, proj_o, edge_o, qkv_o, out_o, up_o, down_o, ggain_o, gshift_o = refs[:10]
    summed, refs = refs[10 : 10 + n], refs[10 + n :]
    act, gin, proj, edge, qkv, out, up, down, in_sem, out_sem = refs
    loads = [
        pltpu.make_async_copy(src, dst, in_sem.at[i])
        for i, (src, dst) in enumerate(zip(held + (act_h, gin_h), summed + (act, gin), strict=True))
    ]
    for load in loads:
        load.start()
    ggain_o[...] = ggain_h[...]
    gshift_o[...] = gshift_h[...]
    stores = []

    def store(src, dst):
        copy = pltpu.make_async_copy(src, dst, out_sem.at[len(stores)])
        copy.start()
        stores.append(copy)

    def widen(dst, l, g, at, first=0, last=None):
        rows = dst.shape[1]
        for c in range(first, dst.shape[2] // 128 if last is None else last):
            dst[l, :, 128 * c : 128 * (c + 1)] = summed[g][at : at + rows].astype(F32)
            at += rows
        return at

    for g, (name, l, first, rows, _) in enumerate(GROUPS):
        loads[g].wait()
        if name == "early":
            at = widen(out, l, g, 0)
            store(out.at[l], out_o.at[l])
            at = widen(up, l, g, at)
            store(up.at[l], up_o.at[l])
            widen(down, l, g, at)
            store(down.at[l], down_o.at[l])
        elif name == "conv":
            at = widen(proj, l, g, 0)
            store(proj.at[l], proj_o.at[l])
            widen(edge, l, g, at)
            store(edge.at[l], edge_o.at[l])
        else:
            widen(qkv, l, g, 0, first // 256, (first + rows) // 256)
            if first + rows == 1536:
                store(qkv.at[l], qkv_o.at[l])
    for i, (src, dst) in enumerate(((act, act_o), (gin, gin_o))):
        loads[n + i].wait()
        store(src, dst)
    for copy in stores:
        copy.wait()


def fused_device(
    N, M, node_input, edge_feat, graph_ids, edge_src, edge_dst, halo_send, w_proj, w_edge, w_qkv,
    w_out, w_up, w_down, norm_gain, norm_shift, cotangent,
):
    R, D = node_input.shape
    E = edge_feat.shape[0]
    L = w_proj.shape[0]
    names = scratch_list(N, M, L, R, E)
    vmem = pl.BlockSpec(memory_space=pltpu.VMEM)
    hbm = pl.BlockSpec(memory_space=pltpu.HBM)
    shape = jax.ShapeDtypeStruct
    rows = shape((R, D), F32)
    norm = shape((3, L, D), F32)
    groups = [shape((rows_g, 128), BF16) for _, _, _, rows_g, _ in GROUPS]
    outs = pl.pallas_call(
        functools.partial(kernel, N, M, L, tuple(names)),
        out_shape=[rows, rows, *groups, norm, norm],
        in_specs=[hbm] + [vmem] * 4 + [hbm] * 7 + [vmem] * 2 + [hbm],
        out_specs=[hbm] * (2 + len(GROUPS)) + [vmem] * 2,
        scratch_shapes=list(names.values()),
        compiler_params=pltpu.CompilerParams(
            collective_id=0, has_side_effects=True, vmem_limit_bytes=60 << 20
        ),
        name="layers",
    )(node_input, graph_ids, edge_src, edge_dst, halo_send, edge_feat, w_proj, w_edge, w_qkv, w_out, w_up,
      w_down, norm_gain.transpose(1, 0, 2), norm_shift.transpose(1, 0, 2), cotangent)
    weights = [shape(w.shape, F32) for w in (w_proj, w_edge, w_qkv, w_out, w_up, w_down)]
    results = pl.pallas_call(
        finish_kernel,
        out_shape=[rows, rows, *weights, norm, norm],
        in_specs=[hbm] * (2 + len(GROUPS)) + [vmem] * 2,
        out_specs=[hbm] * 8 + [vmem] * 2,
        scratch_shapes=[pltpu.VMEM(s.shape, s.dtype) for s in (*groups, rows, rows, *weights)]
        + [pltpu.SemaphoreType.DMA((len(GROUPS) + 2,)), pltpu.SemaphoreType.DMA((14,))],
        compiler_params=pltpu.CompilerParams(vmem_limit_bytes=60 << 20),
        name="gradients",
    )(*outs)
    ggain, gshift = results[8].transpose(1, 0, 2), results[9].transpose(1, 0, 2)
    return (*results[:8], ggain, gshift)


BLOCK_CAP = 2048


def extended_2(block, sides, width):
    for axis, dim in sides:
        count = lax.axis_size(axis)
        forward = [(i, i + 1) for i in range(count - 1)]
        forward.append((count - 1, 0))
        backward = [(target, source) for source, target in forward]
        low = lax.ppermute(
            lax.slice_in_dim(block, block.shape[dim] - width, None, axis=dim), axis, forward
        )
        high = lax.ppermute(lax.slice_in_dim(block, 0, width, axis=dim), axis, backward)
        block = jnp.concatenate([low, block, high], axis=dim)
    return block


def block_length(total_rows, upper_limit):
    for length in range(min(total_rows, upper_limit), 0, -1):
        if total_rows % length == 0:
            return length
    return 1


def outer_product(left, right):
    return lax.dot_general(
        left, right, (((0,), (0,)), ((), ())), preferred_element_type=jnp.float32
    )


def times_transposed(left, weight):
    return lax.dot_general(
        left, weight, (((1,), (1,)), ((), ())), preferred_element_type=jnp.float32
    )


def forward_product(left, weight):
    return jnp.dot(left, weight, preferred_element_type=jnp.float32)


def silu_slope_plain(inputs):
    logistic = jax.nn.sigmoid(inputs)
    return logistic * (1.0 + inputs * (1.0 - logistic))


def normalize(inputs, gain_row, shift_row, node_total):
    batch_mean = lax.psum(jnp.sum(inputs, 0), ("nodes", "rep")) / node_total
    centred = inputs - batch_mean
    batch_var = lax.psum(jnp.sum(centred * centred, 0), ("nodes", "rep")) / node_total
    inv_std = lax.rsqrt(batch_var + NORM_EPS)
    standard = (inputs - batch_mean) * inv_std
    return (standard * gain_row + shift_row, standard, inv_std)


def normalize_back(grad_out, standard, inv_std, gain_row, node_total):
    shift_grad, gain_grad = lax.psum(
        (jnp.sum(grad_out, 0), jnp.sum(grad_out * standard, 0)), ("nodes", "rep")
    )
    grad_in = (
        gain_row
        * inv_std
        * (grad_out - shift_grad / node_total - standard * gain_grad / node_total)
    )
    return (grad_in, gain_grad, shift_grad)


def exchange_sources(outgoing):
    halo_rows = outgoing.shape[0] // 2
    grown = extended_2(outgoing, (("nodes", 0),), halo_rows)
    return jnp.concatenate([grown[:halo_rows], grown[3 * halo_rows :]], 0)


def return_sources(incoming_grad):
    halo_rows = incoming_grad.shape[0] // 2
    grown = extended_2(incoming_grad.astype(jnp.bfloat16), (("nodes", 0),), halo_rows).astype(
        incoming_grad.dtype
    )
    return jnp.concatenate([grown[:halo_rows], grown[3 * halo_rows :]], 0)


def attend_forward(query_rows, key_rows, value_rows, local_graphs, group_graphs):
    row_count = query_rows.shape[0]
    score_scale = HEAD_DIM ** (-0.5)
    queries = query_rows.reshape(row_count, HEADS, HEAD_DIM)

    def add_piece(carried, kv_piece, first_row):
        key_piece, value_piece = kv_piece
        piece_rows = key_piece.shape[0]
        block_len = block_length(piece_rows, BLOCK_CAP)

        def add_block(block_state, block_index):
            row_max, row_sum, accumulated = block_state
            block_start = block_index * block_len
            key_block = lax.dynamic_slice_in_dim(key_piece, block_start, block_len, 0).reshape(
                block_len, HEADS, HEAD_DIM
            )
            value_block = lax.dynamic_slice_in_dim(value_piece, block_start, block_len, 0).reshape(
                block_len, HEADS, HEAD_DIM
            )
            key_graphs = lax.dynamic_slice_in_dim(
                group_graphs, first_row + block_start, block_len, 0
            )
            same_graph = (local_graphs[:, None] == key_graphs[None, :])[None]
            scores = (
                jnp.einsum("qhd,khd->hqk", queries, key_block, preferred_element_type=jnp.float32)
                * score_scale
            )
            scores = jnp.where(same_graph, scores, NEG)
            new_max = jnp.maximum(row_max, jnp.max(scores, 2))
            weights = jnp.where(same_graph, jnp.exp(scores - new_max[:, :, None]), 0.0)
            factor = jnp.exp(row_max - new_max)
            row_sum = row_sum * factor + jnp.sum(weights, 2)
            contrib = jnp.einsum(
                "hqk,khd->qhd",
                weights.astype(jnp.bfloat16),
                value_block,
                preferred_element_type=jnp.float32,
            )
            accumulated = accumulated * jnp.transpose(factor)[:, :, None] + contrib
            return ((new_max, row_sum, accumulated), None)

        carried, _ = lax.scan(add_block, carried, jnp.arange(piece_rows // block_len))
        return carried

    start_state = (
        jnp.full((HEADS, row_count), NEG, jnp.float32),
        jnp.zeros((HEADS, row_count), jnp.float32),
        jnp.zeros((row_count, HEADS, HEAD_DIM), jnp.float32),
    )
    row_max, row_sum, accumulated = add_piece(
        start_state,
        (
            lax.all_gather(key_rows, "nodes", axis=0, tiled=True),
            lax.all_gather(value_rows, "nodes", axis=0, tiled=True),
        ),
        jnp.int32(0),
    )
    attn_raw = accumulated / jnp.transpose(row_sum)[:, :, None]
    log_sum = row_max + jnp.log(row_sum)
    return (attn_raw, log_sum)


def attend_backward(
    query_rows, key_rows, value_rows, grad_low, attn_raw, log_sum, local_graphs, group_graphs
):
    row_count = query_rows.shape[0]
    model_width = HEADS * HEAD_DIM
    score_scale = HEAD_DIM ** (-0.5)
    queries = query_rows.reshape(row_count, HEADS, HEAD_DIM)
    grad_heads = grad_low.reshape(row_count, HEADS, HEAD_DIM)
    row_delta = jnp.einsum("qhd,qhd->hq", grad_heads.astype(jnp.float32), attn_raw)

    def score_block(key_block, value_block, key_graphs):
        same_graph = (local_graphs[:, None] == key_graphs[None, :])[None]
        scores = (
            jnp.einsum("qhd,khd->hqk", queries, key_block, preferred_element_type=jnp.float32)
            * score_scale
        )
        attn_weights = jnp.exp(jnp.where(same_graph, scores - log_sum[:, :, None], NEG))
        grad_weights = jnp.einsum(
            "qhd,khd->hqk", grad_heads, value_block, preferred_element_type=jnp.float32
        )
        grad_scores = (attn_weights * (grad_weights - row_delta[:, :, None])).astype(jnp.bfloat16)
        return (attn_weights, grad_scores)

    def key_terms(attn_weights, grad_scores, block_len):
        grad_keys = (
            jnp.einsum("hqk,qhd->khd", grad_scores, queries, preferred_element_type=jnp.float32)
            * score_scale
        )
        grad_values = jnp.einsum(
            "hqk,qhd->khd",
            attn_weights.astype(jnp.bfloat16),
            grad_heads,
            preferred_element_type=jnp.float32,
        )
        return jnp.concatenate(
            [
                grad_keys.reshape(block_len, model_width),
                grad_values.reshape(block_len, model_width),
            ],
            1,
        )

    def query_term(grad_scores, key_block):
        return (
            jnp.einsum("hqk,khd->qhd", grad_scores, key_block, preferred_element_type=jnp.float32)
            * score_scale
        )

    group_rows = group_graphs.shape[0]

    def add_piece(carried, kv_piece, first_row):
        key_piece, value_piece = kv_piece
        piece_rows = key_piece.shape[0]
        block_len = block_length(piece_rows, BLOCK_CAP)

        def add_block(block_state, block_index):
            grad_query, buffer = block_state
            block_start = block_index * block_len
            key_block = lax.dynamic_slice_in_dim(key_piece, block_start, block_len, 0).reshape(
                block_len, HEADS, HEAD_DIM
            )
            value_block = lax.dynamic_slice_in_dim(value_piece, block_start, block_len, 0).reshape(
                block_len, HEADS, HEAD_DIM
            )
            place = first_row + block_start
            key_graphs = lax.dynamic_slice_in_dim(group_graphs, place, block_len, 0)
            attn_weights, grad_scores = score_block(key_block, value_block, key_graphs)
            grad_query = grad_query + query_term(grad_scores, key_block)
            block_terms = key_terms(attn_weights, grad_scores, block_len)
            current = lax.dynamic_slice_in_dim(buffer, place, block_len, 0)
            buffer = lax.dynamic_update_slice_in_dim(buffer, current + block_terms, place, 0)
            return ((grad_query, buffer), None)

        carried, _ = lax.scan(add_block, carried, jnp.arange(piece_rows // block_len))
        return carried

    start_state = (
        jnp.zeros((row_count, HEADS, HEAD_DIM), jnp.float32),
        jnp.zeros((group_rows, 2 * model_width), jnp.float32),
    )
    grad_query, buffer = add_piece(
        start_state,
        (
            lax.all_gather(key_rows, "nodes", axis=0, tiled=True),
            lax.all_gather(value_rows, "nodes", axis=0, tiled=True),
        ),
        jnp.int32(0),
    )
    grad_kv = lax.psum_scatter(buffer, "nodes", scatter_dimension=0, tiled=True)
    return (
        grad_query.reshape(row_count, model_width),
        grad_kv[:, :model_width],
        grad_kv[:, model_width:],
    )


def layer_forward(
    hidden, params, edge_feat, edge_src, edge_dst, halo_send, local_graphs, group_graphs, node_total
):
    w_proj, w_edge, w_qkv, w_out, w_up, w_down, norm_gains, norm_shifts = params
    row_count, model_width = hidden.shape
    hidden_low = hidden.astype(jnp.bfloat16)
    projected = forward_product(hidden_low, w_proj)
    self_term = projected[:, :model_width]
    dest_term = projected[:, 2 * model_width : 3 * model_width]
    source_rows = jnp.concatenate(
        [projected[:, model_width : 2 * model_width], projected[:, 3 * model_width :]], 1
    ).astype(jnp.bfloat16)
    incoming = exchange_sources(source_rows[halo_send])
    extended = jnp.concatenate([source_rows, incoming], 0)
    edge_rows = extended[edge_src].astype(jnp.float32)
    source_b = edge_rows[:, :model_width]
    source_e = edge_rows[:, model_width:]
    edge_proj = forward_product(edge_feat, w_edge)
    gating = jax.nn.sigmoid(dest_term[edge_dst] + source_e + edge_proj)
    numerator = jax.ops.segment_sum(gating * source_b, edge_dst, row_count)
    denominator = jax.ops.segment_sum(gating, edge_dst, row_count)
    message = self_term + numerator / (denominator + GATE_EPS)
    normed_one, standard_one, inv_one = normalize(
        message, norm_gains[0], norm_shifts[0], node_total
    )
    local_out = hidden + jax.nn.silu(normed_one)
    qkv_low = forward_product(hidden_low, w_qkv).astype(jnp.bfloat16)
    query_rows = qkv_low[:, :model_width]
    key_rows = qkv_low[:, model_width : 2 * model_width]
    value_rows = qkv_low[:, 2 * model_width :]
    attn_raw, log_sum = attend_forward(query_rows, key_rows, value_rows, local_graphs, group_graphs)
    attn_low = attn_raw.reshape(row_count, model_width).astype(jnp.bfloat16)
    attn_proj = forward_product(attn_low, w_out)
    normed_two, standard_two, inv_two = normalize(
        hidden + attn_proj, norm_gains[1], norm_shifts[1], node_total
    )
    mixed = local_out + normed_two
    mixed_low = mixed.astype(jnp.bfloat16)
    up_proj = forward_product(mixed_low, w_up)
    activated = jax.nn.silu(up_proj).astype(jnp.bfloat16)
    down_proj = forward_product(activated, w_down)
    normed_three, standard_three, inv_three = normalize(
        mixed + down_proj, norm_gains[2], norm_shifts[2], node_total
    )
    saved = (
        hidden_low,
        source_b,
        gating,
        numerator,
        denominator,
        normed_one,
        standard_one,
        inv_one,
        query_rows,
        key_rows,
        value_rows,
        attn_raw,
        log_sum,
        attn_low,
        standard_two,
        inv_two,
        mixed_low,
        up_proj,
        activated,
        standard_three,
        inv_three,
    )
    return (normed_three, saved)


def layer_backward(
    grad_out,
    params,
    saved,
    edge_feat,
    edge_src,
    edge_dst,
    halo_send,
    local_graphs,
    group_graphs,
    node_total,
):
    w_proj, w_edge, w_qkv, w_out, w_up, w_down, norm_gains, norm_shifts = params
    (
        hidden_low,
        source_b,
        gating,
        numerator,
        denominator,
        normed_one,
        standard_one,
        inv_one,
        query_rows,
        key_rows,
        value_rows,
        attn_raw,
        log_sum,
        attn_low,
        standard_two,
        inv_two,
        mixed_low,
        up_proj,
        activated,
        standard_three,
        inv_three,
    ) = saved
    row_count, model_width = grad_out.shape
    grad_three, gain_three, shift_three = normalize_back(
        grad_out, standard_three, inv_three, norm_gains[2], node_total
    )
    down_grad = grad_three.astype(jnp.bfloat16)
    grad_w_down = outer_product(activated, down_grad)
    up_grad = (times_transposed(down_grad, w_down) * silu_slope_plain(up_proj)).astype(jnp.bfloat16)
    grad_w_up = outer_product(mixed_low, up_grad)
    grad_mixed = grad_three + times_transposed(up_grad, w_up)
    grad_two, gain_two, shift_two = normalize_back(
        grad_mixed, standard_two, inv_two, norm_gains[1], node_total
    )
    out_grad = grad_two.astype(jnp.bfloat16)
    grad_w_out = outer_product(attn_low, out_grad)
    attn_grad = times_transposed(out_grad, w_out).astype(jnp.bfloat16)
    grad_query, grad_key, grad_value = attend_backward(
        query_rows, key_rows, value_rows, attn_grad, attn_raw, log_sum, local_graphs, group_graphs
    )
    qkv_grad = jnp.concatenate([grad_query, grad_key, grad_value], 1).astype(jnp.bfloat16)
    grad_w_qkv = outer_product(hidden_low, qkv_grad)
    grad_message, gain_one, shift_one = normalize_back(
        grad_mixed * silu_slope_plain(normed_one), standard_one, inv_one, norm_gains[0], node_total
    )
    shifted = denominator + GATE_EPS
    grad_numer = grad_message / shifted
    grad_denom = -grad_message * numerator / (shifted * shifted)
    numer_edge = grad_numer[edge_dst]
    grad_gate = numer_edge * source_b + grad_denom[edge_dst]
    grad_pre_edge = grad_gate * gating * (1.0 - gating)
    edge_grad = grad_pre_edge.astype(jnp.bfloat16)
    grad_w_edge = outer_product(edge_feat, edge_grad)
    grad_dest = jax.ops.segment_sum(grad_pre_edge, edge_dst, row_count)
    grad_extended = jax.ops.segment_sum(
        jnp.concatenate([numer_edge * gating, grad_pre_edge], 1),
        edge_src,
        row_count + halo_send.shape[0],
    )
    returned = return_sources(grad_extended[row_count:])
    grad_source = grad_extended[:row_count].at[halo_send].add(returned)
    proj_grad = jnp.concatenate(
        [grad_message, grad_source[:, :model_width], grad_dest, grad_source[:, model_width:]], 1
    ).astype(jnp.bfloat16)
    grad_w_proj = outer_product(hidden_low, proj_grad)
    grad_hidden = (
        grad_mixed
        + grad_two
        + times_transposed(proj_grad, w_proj)
        + times_transposed(qkv_grad, w_qkv)
    )
    weight_grads = (grad_w_proj, grad_w_edge, grad_w_qkv, grad_w_out, grad_w_up, grad_w_down)
    return (
        grad_hidden,
        weight_grads,
        jnp.stack([gain_one, gain_two, gain_three]),
        jnp.stack([shift_one, shift_two, shift_three]),
    )


def per_device(
    node_input,
    edge_feat,
    graph_ids,
    edge_src,
    edge_dst,
    halo_send,
    w_proj,
    w_edge,
    w_qkv,
    w_out,
    w_up,
    w_down,
    norm_gain,
    norm_shift,
    cotangent,
):
    group_graphs = lax.all_gather(graph_ids, "nodes", axis=0, tiled=True)
    node_total = node_input.shape[0] * lax.axis_size("nodes") * lax.axis_size("rep")
    layer_count = w_proj.shape[0]
    layer_params = [
        (
            w_proj[layer_index],
            w_edge[layer_index],
            w_qkv[layer_index],
            w_out[layer_index],
            w_up[layer_index],
            w_down[layer_index],
            norm_gain[layer_index],
            norm_shift[layer_index],
        )
        for layer_index in range(layer_count)
    ]
    hidden = node_input.astype(jnp.float32)
    saved_all = []
    for layer_index in range(layer_count):
        hidden, saved = layer_forward(
            hidden,
            layer_params[layer_index],
            edge_feat,
            edge_src,
            edge_dst,
            halo_send,
            graph_ids,
            group_graphs,
            node_total,
        )
        saved_all.append(saved)
    grad_hidden = cotangent.astype(jnp.float32)
    weight_parts = [None] * layer_count
    gain_parts = [None] * layer_count
    shift_parts = [None] * layer_count
    for layer_index in range(layer_count - 1, -1, -1):
        (
            grad_hidden,
            weight_parts[layer_index],
            gain_parts[layer_index],
            shift_parts[layer_index],
        ) = layer_backward(
            grad_hidden,
            layer_params[layer_index],
            saved_all[layer_index],
            edge_feat,
            edge_src,
            edge_dst,
            halo_send,
            graph_ids,
            group_graphs,
            node_total,
        )
    proj_local = jnp.stack([weight_parts[layer_index][0] for layer_index in range(layer_count)])
    edge_local = jnp.stack([weight_parts[layer_index][1] for layer_index in range(layer_count)])
    qkv_local = jnp.stack([weight_parts[layer_index][2] for layer_index in range(layer_count)])
    out_local = jnp.stack([weight_parts[layer_index][3] for layer_index in range(layer_count)])
    up_local = jnp.stack([weight_parts[layer_index][4] for layer_index in range(layer_count)])
    down_local = jnp.stack([weight_parts[layer_index][5] for layer_index in range(layer_count)])
    grad_proj, grad_edge, grad_qkv, grad_out, grad_up, grad_down = lax.psum(
        (proj_local, edge_local, qkv_local, out_local, up_local, down_local), ("nodes", "rep")
    )
    return (
        hidden,
        grad_hidden,
        grad_proj,
        grad_edge,
        grad_qkv,
        grad_out,
        grad_up,
        grad_down,
        jnp.stack(gain_parts),
        jnp.stack(shift_parts),
    )


def solution(mesh):
    in_specs = (
        P(("rep", "nodes"), None),
        P(("rep", "nodes"), None),
        P(("rep", "nodes")),
        P(("rep", "nodes")),
        P(("rep", "nodes")),
        P(("rep", "nodes")),
        P(),
        P(),
        P(),
        P(),
        P(),
        P(),
        P(),
        P(),
        P(("rep", "nodes"), None),
    )
    out_specs = (
        P(("rep", "nodes"), None),
        P(("rep", "nodes"), None),
        P(),
        P(),
        P(),
        P(),
        P(),
        P(),
        P(),
        P(),
    )
    N, M = mesh.shape["nodes"], mesh.shape["rep"]
    fused = N in (4, 8) and M % 2 == 0 and 512 % (16 * N * M) == 0
    return jax.shard_map(
        functools.partial(fused_device, N, M) if fused else per_device,
        mesh=mesh, in_specs=in_specs, out_specs=out_specs, check_vma=False,
    )
```

```python
import functools
import math

import jax
import jax.numpy as jnp
from jax import lax
from jax.experimental import pallas as pl
from jax.experimental.pallas import tpu as pltpu
from jax.sharding import PartitionSpec as P

HEADS = 8
HEAD_DIM = 32
NEG = -1e30
NORM_EPS = 1e-05
GATE_EPS = 1e-06
F32, BF16, I32 = jnp.float32, jnp.bfloat16, jnp.int32
MESH = pl.DeviceIdType.MESH
SYNCS = 7
GROUPS = (
    ("early", 1, 0, 2560, ("core", "y", "nodes")),
    ("conv", 1, 0, 2560, ("core", "y", "nodes")),
    ("qkv", 1, 0, 1536, ("core", "y", "nodes")),
    ("early", 0, 0, 2560, ("core", "x", "y", "z")),
    ("conv", 0, 0, 2560, ("core", "y", "x", "z")),
    ("qkv", 0, 0, 1024, ("core", "x", "y", "z")),
    ("qkv", 0, 1024, 512, ("core", "y", "x", "z")),
)
BESIDE, AFTER = (0, 1, 2), (3, 4, 5, 6)


def dot(left, right):
    return lax.dot_general(
        left, right, (((1,), (0,)), ((), ())), preferred_element_type=F32
    )


def dot_nt(left, right):
    return lax.dot_general(
        left, right, (((1,), (1,)), ((), ())), preferred_element_type=F32
    )


def dot_tn(left, right):
    return lax.dot_general(
        left, right, (((0,), (0,)), ((), ())), preferred_element_type=F32
    )


def split(value):
    high = value.astype(BF16)
    return high, (value - high.astype(F32)).astype(BF16)


def select_rows(onehot, value):
    high, low = split(value)
    return dot(onehot, high) + dot(onehot, low)


def sigmoid(value):
    return 1.0 / (1.0 + jnp.exp(-value))


def silu_slope(value):
    logistic = sigmoid(value)
    return logistic * (1.0 + value * (1.0 - logistic))


def col_sum(value):
    return jnp.sum(value, axis=0, keepdims=True)


def pack(first, second, third, fourth):
    halves = []
    for row in (first, second, third, fourth):
        halves += [row[:, :128], row[:, 128:]]
    return jnp.concatenate(halves, 0)


def unpack(tile):
    return [
        jnp.concatenate([tile[2 * i : 2 * i + 1], tile[2 * i + 1 : 2 * i + 2]], 1)
        for i in range(4)
    ]


def combine_pair(tiles, count):
    mean = jnp.mean(tiles[:, 0:4], 0)
    off = tiles[:, 0:4] - mean
    return jnp.concatenate([mean, jnp.sum(tiles[:, 4:8] + count * off * off, 0)], 0)


def combine_last(tiles, count):
    mean = jnp.mean(tiles[:, 0:2], 0)
    off = tiles[:, 0:2] - mean
    return jnp.concatenate(
        [
            mean,
            jnp.sum(tiles[:, 2:4], 0),
            jnp.sum(tiles[:, 4:6] + count * off * off, 0),
            jnp.sum(tiles[:, 6:8] + off * tiles[:, 2:4], 0),
        ],
        0,
    )


def combine_sum(tiles, count):
    return jnp.sum(tiles, 0)


class Refs:
    pass


def axis_sizes(N, M):
    return dict(core=2, y=M // 2, x=2, z=N // 2, rep=M, nodes=N)


def group_scratch(N, M, groups):
    vm = lambda dtype, *shape: pltpu.VMEM(shape, dtype)
    sizes, names = axis_sizes(N, M), {}
    for g in groups:
        _, _, _, rows, stages = GROUPS[g]
        names[f"go{g}"] = vm(BF16, rows, 128)
        left = rows
        for k, axis in enumerate(stages):
            left //= sizes[axis]
            names[f"ga{g}_{k}"] = vm(BF16, sizes[axis] - 1, left, 128)
            if k < len(stages) - 1:
                names[f"gh{g}_{k}"] = vm(BF16, left, 128)
    return names


def scratch_list(N, M, L, R, E):
    NZ, NB, G = N // 2, N // 4, N * R
    D, FF, W, HH = 256, 512, 4 * R, HEADS // 2 * R
    dma = lambda *shape: pltpu.SemaphoreType.DMA(shape)
    vm = lambda dtype, *shape: pltpu.VMEM(shape, dtype)
    names = dict(
        gb=vm(BF16, L, N, R, D),
        xs=vm(BF16, L, N, R, D),
        meta=vm(I32, N, 8, 256),
        ef=vm(BF16, E, D),
        cot=vm(BF16, R, D),
        wp=vm(BF16, L, D, 4 * D),
        we=vm(BF16, L, D, D),
        wqkv=vm(BF16, L, D, 3 * D),
        wo=vm(BF16, L, D, D),
        wu=vm(BF16, L, D, FF),
        wd=vm(BF16, L, FF, D),
        st1=vm(F32, SYNCS, M * N, 8, 128),
        gain=vm(F32, L, 8, D),
        shift=vm(F32, L, 8, D),
        ggain=vm(F32, L, 8, D),
        gshift=vm(F32, L, 8, D),
        iv=vm(F32, L, 8, D),
        moff=vm(F32, N, 8, D),
        move=vm(F32, 8, D),
        T=vm(BF16, E, R),
        TT=vm(BF16, R, E),
        S=vm(BF16, E, 256),
        ST=vm(BF16, 256, E),
        efT=vm(BF16, D, E),
        HP=vm(BF16, 32, R),
        HN=vm(BF16, 32, R),
        A=vm(BF16, R, 64),
        bias=vm(F32, R, G),
        ce=vm(F32, L, E, D),
        xf=vm(F32, L + 1, R, D),
        xe=vm(BF16, L, 256, D),
        xeT=vm(BF16, D, 256),
        gate=vm(F32, L, E, D),
        bs=vm(BF16, L, E, D),
        num=vm(F32, L, R, D),
        den=vm(F32, L, R, D),
        z0=vm(F32, L, R, D),
        z1=vm(F32, L, R, D),
        z2=vm(F32, L, R, D),
        kk=vm(BF16, L, G, D),
        vv=vm(BF16, L, G, D),
        kT=vm(BF16, D, G),
        vT=vm(BF16, D, G),
        od=vm(F32, NB, R, D),
        md=vm(F32, NB, R, D),
        ld=vm(F32, NB, R, D),
        rb=vm(F32, L, NB, R, D),
        pst=vm(BF16, L, HEADS * R, G),
        oraw=vm(F32, L, R, D),
        ob=vm(BF16, L, R, D),
        mb=vm(BF16, L, R, D),
        u=vm(F32, L, R, FF),
        g=vm(BF16, L, R, FF),
        dy=vm(F32, R, D),
        dmix=vm(F32, R, D),
        dxo=vm(F32, R, D),
        dob=vm(F32, R, D),
        dq=vm(F32, R, D),
        qm=vm(BF16, L, 2, HH, 128),
        qmT=vm(BF16, 2, 128, HH),
        dom=vm(BF16, HH, 128),
        dss=vm(BF16, HH, W),
        dkv=vm(BF16, 2 * D, W),
        gkv=vm(F32, 2 * D, D),
        dce=vm(BF16, E, D),
        dproj=vm(BF16, 4, 256, D),
        dxs=vm(BF16, L, NZ, 2, R, D),
        rs1=vm(BF16, L, NZ, R, D),
        cs=vm(BF16, L, NZ, R, D),
        rs2=vm(BF16, L, NZ, R, D),
        ro=vm(BF16, L, 3, R, D),
        hs=vm(BF16, L, 2, 32, D),
        hr=vm(BF16, L, 2, 32, D),
    )
    names.update(
        gs_early=vm(BF16, L, 2560, 128),
        gs_conv=vm(BF16, L, 2560, 128),
        gs_qkv=vm(BF16, L, 1536, 128),
    )
    names.update(group_scratch(N, M, BESIDE))
    names.update(
        ar_s=dma(len(GROUPS), 8),
        ar_r=dma(len(GROUPS), 8),
        ar_l=dma(len(GROUPS)),
        load=dma(10),
        store=dma(5),
        meta_s=dma(1),
        meta_r=dma(1),
        st1_s=dma(SYNCS),
        st1_r=dma(SYNCS),
        agc_s=dma(L, NZ),
        agc_r=dma(L, NZ),
        agp_s=dma(L, NZ),
        agp_r=dma(L, NZ),
        rsp_s=dma(L, NZ),
        rsp_r=dma(L, NZ),
        ro_s=dma(L, 3),
        ro_r=dma(L, 3),
        rsc_s=dma(L, NZ),
        rsc_r=dma(L, NZ),
        hal_s=dma(L, 2),
        hal_r=dma(L, 2),
    )
    return names


IN_NAMES = (
    "x_in", "ids", "edge_src", "edge_dst", "halo", "ef_h", "wp_h", "we_h", "wqkv_h", "wo_h", "wu_h", "wd_h",
    "gain_in", "shift_in", "cot_h",
)
OUT_NAMES = (
    "out_act", "grad_in", *(f"gout{g}" for g in BESIDE), "early_out", "conv_out", "qkv_out", "ggain_out", "gshift_out",
)


def reducers(r_, N, M, send_rows, arrive, sent):
    me = lax.axis_index("nodes")
    rep = lax.axis_index("rep")
    z, par = me // 2, me % 2
    sizes = axis_sizes(N, M)
    core, row = rep % 2, rep // 2
    places = dict(
        core=(core, lambda t: dict(rep=2 * row + t)),
        y=(row, lambda t: dict(rep=2 * t + core)),
        x=(par, lambda t: dict(nodes=2 * z + t)),
        z=(z, lambda t: dict(nodes=2 * t + par)),
        rep=(rep, lambda t: dict(rep=t)),
        nodes=(me, lambda t: dict(nodes=t)),
    )

    def reduce_step(g, step):
        name, layer, first, rows, stages = GROUPS[g]
        K = len(stages)
        gs, out = getattr(r_, f"gs_{name}").at[layer, first : first + rows], getattr(r_, f"go{g}")
        count, offset = [rows], [0]
        for axis in stages:
            count.append(count[-1] // sizes[axis])
            offset.append(offset[-1] + places[axis][0] * count[-1])
        take = lambda start, size: pl.ds(pl.multiple_of(start, 16), size)
        if 1 <= step <= K:
            k = step - 1
            got = getattr(r_, f"ga{g}_{k}")
            arrive(got, r_.ar_r.at[g, k])
            held = gs if k == 0 else getattr(r_, f"gh{g}_{k - 1}")
            index = places[stages[k]][0]
            acc = held[take(index * count[k + 1], count[k + 1])].astype(F32)
            for slot in range(sizes[stages[k]] - 1):
                acc = acc + got[slot].astype(F32)
            if step < K:
                getattr(r_, f"gh{g}_{k}")[...] = acc.astype(BF16)
            else:
                out[take(offset[K], count[K])] = acc.astype(BF16)
        elif step > K:
            k = 2 * K - step
            arrive(out.at[0 : (sizes[stages[k]] - 1) * count[k + 1]], r_.ar_r.at[g, step - 1])
        if step < K:
            held = gs if step == 0 else getattr(r_, f"gh{g}_{step - 1}")
            index, device = places[stages[step]]
            size = sizes[stages[step]]
            for d in range(1, size):
                to = (index + d) % size
                send_rows(held.at[take(to * count[step + 1], count[step + 1])], getattr(r_, f"ga{g}_{step}").at[d - 1],
                     count[step + 1], r_.ar_s.at[g, step], r_.ar_r.at[g, step], **device(to))
        elif step < 2 * K:
            k = 2 * K - 1 - step
            index, device = places[stages[k]]
            size = sizes[stages[k]]
            here = out.at[take(offset[k + 1], count[k + 1])]
            for d in range(1, size):
                send_rows(here, here, count[k + 1], r_.ar_s.at[g, step], r_.ar_r.at[g, step],
                          **device((index + d) % size))
        else:
            pltpu.make_async_copy(out, getattr(r_, f"gout{g}"), r_.ar_l.at[g]).start()

    def reduce_drain(g):
        _, _, _, rows, stages = GROUPS[g]
        K, left = len(stages), rows
        out = getattr(r_, f"go{g}")
        for k, axis in enumerate(stages):
            left //= sizes[axis]
            for step in (k, 2 * K - 1 - k):
                sent(out.at[0 : (sizes[axis] - 1) * left], r_.ar_s.at[g, step])
        pltpu.make_async_copy(out, getattr(r_, f"gout{g}"), r_.ar_l.at[g]).wait()

    return reduce_step, reduce_drain


def senders(partner):
    def remote(src, dst, s_sem, r_sem, **where):
        return pltpu.make_async_remote_copy(
            src_ref=src, dst_ref=dst, send_sem=s_sem, recv_sem=r_sem,
            device_id=where, device_id_type=MESH,
        )

    def send(src, dst, s_sem, r_sem, **where):
        remote(src, dst, s_sem, r_sem, **where).start()

    def send_rows(src, dst, rows, s_sem, r_sem, **where):
        pieces = next(p for p in range(1, rows) if rows % (16 * p) == 0 and rows // p <= 128)
        for at in range(0, rows, rows // pieces):
            cut = pl.ds(at, rows // pieces)
            send(src.at[cut], dst.at[cut], s_sem, r_sem, **where)

    def arrive(dst, r_sem):
        remote(dst, dst, r_sem, r_sem, nodes=partner).wait_recv()

    def sent(src, s_sem):
        remote(src, src, s_sem, s_sem, nodes=partner).wait_send()

    return send, send_rows, arrive, sent


def enter(N, M):
    me = lax.axis_index("nodes")
    rep = lax.axis_index("rep")
    barrier = pltpu.get_barrier_semaphore()
    for dr in range(M):
        for d in range(N):
            if dr + d > 0:
                pl.semaphore_signal(barrier, inc=1, device_id={"rep": (rep + dr) % M, "nodes": (me + d) % N},
                                    device_id_type=MESH)
    pl.semaphore_wait(barrier, M * N - 1)


def kernel(N, M, L, names, *args):
    r_ = Refs()
    for name, ref in zip(IN_NAMES + OUT_NAMES + tuple(names), args, strict=True):
        setattr(r_, name, ref)
    R, D = r_.x_in.shape
    E = r_.ef.shape[0]
    NZ, NB, G, W = N // 2, N // 4, N * R, 4 * R
    HK = HEADS // 2
    total = float(N * M * R)
    scale = HEAD_DIM ** -0.5
    me = lax.axis_index("nodes")
    rep = lax.axis_index("rep")
    z = me // 2
    par = me % 2
    partner = 2 * z + (1 - par)
    prev = (me + N - 1) % N
    nxt = (me + 1) % N
    zh, zl = z // 2, z % 2
    z_to = lambda t: 2 * ((zh + t // 2) % NB) + (zl + t % 2) % 2
    z_from = lambda t: 2 * ((zh + NB - t // 2) % NB) + (zl + t % 2) % 2

    send, send_rows, arrive, sent = senders(partner)

    def when(condition, *acts):
        @pl.when(condition)
        def _():
            for act in acts:
                act()

    loads = [
        pltpu.make_async_copy(getattr(r_, f"{name}_h"), getattr(r_, name), r_.load.at[i])
        for i, name in enumerate(("ef", "we", "wqkv", "wp", "wo", "wu", "wd", "cot"))
    ]
    own_rows = pltpu.make_async_copy(r_.x_in, r_.gb.at[0, me], r_.load.at[8])
    own_rows.start()
    for load in loads:
        load.start()

    enter(N, M)

    def gather_start(l):
        mine = r_.gb.at[l, me]
        send_rows(mine, mine, R, r_.agp_s.at[l, 0], r_.agp_r.at[l, 0], nodes=partner)
        send_rows(mine, mine, R, r_.agc_s.at[l, 1], r_.agc_r.at[l, 1], nodes=2 * z_to(1) + par)
        send_rows(mine, mine, R, r_.agp_s.at[l, 1], r_.agp_r.at[l, 1], nodes=2 * z_to(1) + 1 - par)
        for t in range(2, NZ):
            send_rows(mine, mine, R, r_.agc_s.at[l, t], r_.agc_r.at[l, t], nodes=2 * z_to(t) + par)

    def gather_pass(l, t):
        piece = r_.gb.at[l, 2 * z_from(t) + par]
        arrive(piece, r_.agc_r.at[l, t])
        send_rows(piece, piece, R, r_.agp_s.at[l, t], r_.agp_r.at[l, t], nodes=partner)

    def gather_take(l, t):
        arrive(r_.gb.at[l, 2 * z_from(t) + 1 - par], r_.agp_r.at[l, t])

    def sync_start(k, tile):
        mine = rep * N + me
        r_.st1[k, mine] = tile
        for dr in range(M):
            for d in range(N):
                if dr + d > 0:
                    send(r_.st1.at[k, mine], r_.st1.at[k, mine], r_.st1_s.at[k], r_.st1_r.at[k],
                         rep=(rep + dr) % M, nodes=(me + d) % N)

    def sync_finish(k, combine):
        arrive(r_.st1.at[k, 0 : M * N - 1], r_.st1_r.at[k])
        return unpack(combine(r_.st1[k], float(R)))

    reduce_step, reduce_drain = reducers(r_, N, M, send_rows, arrive, sent)

    def put(buf, l, at, value):
        rows = value.shape[0]
        for c in range(value.shape[1] // 128):
            buf[l, at : at + rows] = value[:, 128 * c : 128 * (c + 1)].astype(BF16)
            at += rows
        return at

    lane_head = lax.broadcasted_iota(I32, (R, 128), 1) // HEAD_DIM

    def by_head(parts):
        out = parts[0]
        for k in range(1, HK):
            out = jnp.where(lane_head == k, parts[k], out)
        return out

    r_.meta[me] = jnp.full((8, 256), -1, I32)
    r_.meta[me, 0:1, 0:R] = r_.ids[...].reshape(1, R)
    r_.meta[me, 1:2, 0:48] = r_.halo[...].reshape(1, 48)
    for d in range(1, N):
        send(r_.meta.at[me], r_.meta.at[me], r_.meta_s.at[0], r_.meta_r.at[0], nodes=(me + d) % N)
    own_rows.wait()
    gather_start(0)

    src_row = r_.edge_src[...].reshape(1, E)
    src_row = jnp.where(src_row < R + 24, src_row, src_row + 8)
    dst_row = r_.edge_dst[...].reshape(1, E)
    src_col = jnp.broadcast_to(src_row, (128, E)).T[:, 0:1]
    dst_col = jnp.broadcast_to(dst_row, (128, E)).T[:, 0:1]
    as_mask = lambda cond: cond.astype(F32).astype(BF16)
    r_.T[...] = as_mask(dst_col == lax.broadcasted_iota(I32, (E, R), 1))
    r_.TT[...] = as_mask(dst_row == lax.broadcasted_iota(I32, (R, E), 0))
    r_.S[...] = as_mask(src_col == lax.broadcasted_iota(I32, (E, 256), 1))
    r_.ST[...] = as_mask(src_row == lax.broadcasted_iota(I32, (256, E), 0))
    loads[0].wait()
    r_.efT[...] = r_.ef[...].T
    loads[1].wait()
    for l in range(L):
        r_.ce[l] = dot(r_.ef[...], r_.we[l])
        for k in range(3):
            r_.gain[l, k : k + 1] = r_.gain_in[k, l : l + 1]
            r_.shift[l, k : k + 1] = r_.shift_in[k, l : l + 1]
    r_.xf[0] = r_.gb[0, me].astype(F32)
    r_.moff[...] = jnp.zeros((N, 8, D), F32)
    r_.move[0:1] = jnp.ones((1, D), F32)
    r_.move[1:2] = jnp.zeros((1, D), F32)
    for load in loads[2:]:
        load.wait()

    arrive(r_.meta.at[0 : N - 1], r_.meta_r.at[0])
    id_col = jnp.broadcast_to(r_.meta[me][0:1, 0:R], (128, R)).T[:, 0:1]
    id_row = jnp.concatenate([r_.meta[j][0:1, 0:R] for j in range(N)], 1)
    r_.bias[...] = jnp.where(id_col == id_row, 0.0, NEG)

    def halo_onehot(device, start):
        col = jnp.broadcast_to(r_.meta[device][1:2, 0:128], (128, 128)).T[start : start + 24, 0:1]
        hot = (col == lax.broadcasted_iota(I32, (24, R), 1)).astype(F32)
        return jnp.concatenate([hot, jnp.zeros((8, R), F32)], 0).astype(BF16)

    r_.HP[...] = halo_onehot(prev, 24)
    r_.HN[...] = halo_onehot(nxt, 0)
    r_.A[...] = as_mask(r_.meta[me][1:2, 0:64] == lax.broadcasted_iota(I32, (R, 64), 0))

    factor_exp = scale * math.log2(math.e)

    def prepare_queries(l):
        q = dot(r_.xs[l, me], r_.wqkv[l, :, :D]).astype(BF16).astype(F32)
        for hf in range(2):
            for k in range(HK):
                part = jnp.where(lane_head == k, q[:, 128 * hf : 128 * (hf + 1)], 0.0)
                r_.qm[l, hf, k * R : (k + 1) * R] = part.astype(BF16)

    def head_rows(hf, k, count=1):
        return pl.ds(pl.multiple_of((hf * HK + k) * R, 64), count * R)

    def lane_half(hf):
        return pl.ds(pl.multiple_of(hf * 128, 128), 128)

    def attention_block(l, i, middle):
        half = (zh + NB - i) % NB
        rows = pl.ds(pl.multiple_of(half * W, 128), W)
        x = r_.xs[l, pl.ds(4 * half, 4)].reshape(W, D)
        key = dot(x, r_.wqkv[l, :, D : 2 * D]).astype(BF16)
        r_.kk[l, rows] = key
        r_.kT[:, rows] = key.T
        r_.vv[l, rows] = dot(x, r_.wqkv[l, :, 2 * D :]).astype(BF16)

        def heads(hf, carry):
            lanes = lane_half(hf)
            tops, sums, outs = [], [], []
            for c in range(HK // 2):
                scores = dot(r_.qm[l, hf, 2 * c * R : 2 * (c + 1) * R], r_.kT[lanes, rows])
                for k in range(2):
                    s = scores[k * R : (k + 1) * R] + r_.bias[:, rows]
                    top = jnp.max(s, 1, keepdims=True)
                    e = jnp.exp2((s - top) * factor_exp)
                    tops.append(top)
                    sums.append(jnp.sum(e, 1, keepdims=True))
                    r_.pst[l, head_rows(hf, 2 * c + k), rows] = e.astype(BF16)
                o = dot(r_.pst[l, head_rows(hf, 2 * c, 2), rows], r_.vv[l, rows, lanes])
                outs += [o[0:R], o[R : 2 * R]]
            r_.md[i, :, lanes] = by_head([jnp.broadcast_to(v, (R, 128)) for v in tops])
            r_.ld[i, :, lanes] = by_head([jnp.broadcast_to(v, (R, 128)) for v in sums])
            r_.od[i, :, lanes] = by_head(outs)
            middle(i, hf)
            return carry

        lax.fori_loop(0, 2, heads, 0)

    def attention_end(l):
        top = r_.md[0]
        for i in range(1, NB):
            top = jnp.maximum(top, r_.md[i])
        factors = [jnp.exp2((r_.md[i] - top) * factor_exp) for i in range(NB)]
        inv = 1.0 / sum(factors[i] * r_.ld[i] for i in range(NB))
        o = jnp.zeros((R, D), F32)
        for i in range(NB):
            r_.rb[l, i] = factors[i] * inv
            o = o + factors[i] * inv * r_.od[i]
        r_.oraw[l] = o
        ob = o.astype(BF16)
        r_.ob[l] = ob
        t1 = r_.xf[l] + dot(ob, r_.wo[l])
        r_.z1[l] = t1
        mean1 = col_sum(t1) / R
        return mean1, col_sum((t1 - mean1) * (t1 - mean1))

    def convolution(l):
        xs = r_.xs
        xb = xs[l, me]
        r_.xe[l, 0:R] = xb
        r_.xe[l, R : R + 32] = dot(r_.HP[...], xs[l, prev]).astype(BF16)
        r_.xe[l, R + 32 : R + 64] = dot(r_.HN[...], xs[l, nxt]).astype(BF16)
        xe = r_.xe[l]
        tab_b = dot(xe, r_.wp[l, :, D : 2 * D]).astype(BF16)
        tab_e = dot(xe, r_.wp[l, :, 3 * D :]).astype(BF16)
        pa = dot(xb, r_.wp[l, :, 0:D])
        pd = dot(xb, r_.wp[l, :, 2 * D : 3 * D])
        bs = dot(r_.S[...], tab_b)
        r_.bs[l] = bs.astype(BF16)
        gate = sigmoid(select_rows(r_.T[...], pd) + dot(r_.S[...], tab_e) + r_.ce[l])
        r_.gate[l] = gate
        num = select_rows(r_.TT[...], gate * bs)
        den = select_rows(r_.TT[...], gate)
        r_.num[l] = num
        r_.den[l] = den
        msg = pa + num / (den + GATE_EPS)
        r_.z0[l] = msg

    def forward(l, carry):
        def ready(js):
            for j in js:
                moved = (r_.gb[l, j].astype(F32) + r_.moff[j, 0:1]) * r_.move[0:1] + r_.move[1:2]
                r_.xs[l, j] = moved.astype(BF16)

        r_.xs[l, me] = r_.xf[l].astype(BF16)
        prepare_queries(l)
        arrive(r_.gb.at[l, 2 * z_from(1) + par], r_.agc_r.at[l, 1])
        gather_take(l, 0)
        gather_take(l, 1)
        ready([partner, 2 * z_from(1) + par, 2 * z_from(1) + 1 - par])

        def middle(i, hf):
            when((i == 0) & (hf == 0), *[functools.partial(gather_pass, l, t) for t in range(2, NZ)])

        def block(i, carry):
            attention_block(l, i, middle)

            @pl.when(i == 0)
            def _():
                for t in range(2, NZ):
                    gather_take(l, t)
                ready([2 * z_from(t) + p for t in range(2, NZ) for p in range(2)])
                convolution(l)

            return carry

        lax.fori_loop(0, NB, block, 0)
        mean1, sq1 = attention_end(l)
        msg = r_.z0[l]
        mean0 = col_sum(msg) / R
        sq0 = col_sum((msg - mean0) * (msg - mean0))
        sync_start(2 * l, pack(mean0, mean1, sq0, sq1))
        mean0, mean1, sq0, sq1 = sync_finish(2 * l, combine_pair)
        inv0 = lax.rsqrt(sq0 / total + NORM_EPS)
        inv1 = lax.rsqrt(sq1 / total + NORM_EPS)
        r_.iv[l, 0:1] = inv0
        r_.iv[l, 1:2] = inv1
        z0 = (r_.z0[l] - mean0) * inv0
        z1 = (r_.z1[l] - mean1) * inv1
        r_.z0[l] = z0
        r_.z1[l] = z1
        n0 = z0 * r_.gain[l, 0:1] + r_.shift[l, 0:1]
        mix = r_.xf[l] + n0 * sigmoid(n0) + z1 * r_.gain[l, 1:2] + r_.shift[l, 1:2]
        mb = mix.astype(BF16)
        r_.mb[l] = mb
        u = dot(mb, r_.wu[l])
        r_.u[l] = u
        g = (u * sigmoid(u)).astype(BF16)
        r_.g[l] = g
        y = mix + dot(g, r_.wd[l])
        r_.z2[l] = y
        mean = col_sum(y) / R
        cent = y - mean
        k = 2 * l + 1
        dy = r_.cot[...].astype(F32)
        sync_start(k, pack(mean, col_sum(dy), col_sum(cent * cent), col_sum(dy * cent)))

        @pl.when(l < L - 1)
        def _():
            r_.gb[l + 1, me] = cent.astype(BF16)
            gather_start(l + 1)

        tot_mean, dy_sum, tot_sq, dy_cent = sync_finish(k, combine_last)
        inv2 = lax.rsqrt(tot_sq / total + NORM_EPS)
        r_.iv[l, 2:3] = inv2
        z2 = (r_.z2[l] - tot_mean) * inv2
        r_.z2[l] = z2
        gain, shift = r_.gain[l, 2:3], r_.shift[l, 2:3]
        r_.xf[l + 1] = z2 * gain + shift
        r_.gshift[l, 2:3] = dy_sum
        r_.ggain[l, 2:3] = dy_cent * inv2
        for j in range(N):
            tile = r_.st1[k, rep * N + j]
            r_.moff[j, 0:1] = jnp.concatenate([tile[0:1], tile[1:2]], 1) - tot_mean
        r_.move[0:1] = inv2 * gain
        r_.move[1:2] = shift
        return carry

    lax.fori_loop(0, L, forward, 0)
    act_copy = pltpu.make_async_copy(r_.xf.at[L], r_.out_act, r_.store.at[0])
    act_copy.start()

    def back_feed_forward(l, k):
        s2, g2 = r_.gshift[l, 2:3], r_.ggain[l, 2:3]
        d3 = r_.gain[l, 2:3] * r_.iv[l, 2:3] * (r_.dy[...] - s2 / total - r_.z2[l] * (g2 / total))
        db = d3.astype(BF16)
        dub = (dot_nt(db, r_.wd[l]) * silu_slope(r_.u[l])).astype(BF16)
        dmix = d3 + dot_nt(dub, r_.wu[l])
        r_.dmix[...] = dmix
        n0 = r_.z0[l] * r_.gain[l, 0:1] + r_.shift[l, 0:1]
        gy0 = dmix * silu_slope(n0)
        sync_start(k, pack(col_sum(dmix), col_sum(dmix * r_.z1[l]), col_sum(gy0), col_sum(gy0 * r_.z0[l])))
        at = put(r_.gs_early, l, 512, dot_tn(r_.mb[l], dub))
        put(r_.gs_early, l, at, dot_tn(r_.g[l], db))
        r_.vT[...] = r_.vv[l].T
        r_.xeT[...] = r_.xe[l].T
        for hf in range(2):
            r_.qmT[hf] = r_.qm[l, hf].T

    def back_norms(l, k):
        s1, g1, s0, g0 = sync_finish(k, combine_sum)
        r_.gshift[l, 1:2] = s1
        r_.ggain[l, 1:2] = g1
        r_.gshift[l, 0:1] = s0
        r_.ggain[l, 0:1] = g0
        dmix = r_.dmix[...]
        d2 = r_.gain[l, 1:2] * r_.iv[l, 1:2] * (dmix - s1 / total - r_.z1[l] * (g1 / total))
        dab = d2.astype(BF16)
        r_.dxo[...] = dmix + d2
        r_.dob[...] = dot_nt(dab, r_.wo[l]).astype(BF16).astype(F32)
        put(r_.gs_early, l, 0, dot_tn(r_.ob[l], dab))
        r_.gkv[...] = jnp.zeros((2 * D, D), F32)
        r_.dq[...] = jnp.zeros((R, D), F32)

    def back_attention_block(l, i, between):
        t1 = (i + 1) % NB
        half = (zh + t1) % NB
        rows = pl.ds(pl.multiple_of(half * W, 128), W)

        def heads(hf, carry):
            lanes = lane_half(hf)
            dos = r_.dob[:, lanes] * r_.rb[l, (NB - t1) % NB, :, lanes]
            prod = dos * r_.oraw[l, :, lanes]
            for k in range(HK):
                r_.dom[k * R : (k + 1) * R] = jnp.where(lane_head == k, dos, 0.0).astype(BF16)
            parts = []
            for c in range(HK // 2):
                both = slice(2 * c * R, 2 * (c + 1) * R)
                dp = dot(r_.dom[both], r_.vT[lanes, rows])
                for k in range(2):
                    h = 2 * c + k
                    delta = jnp.sum(jnp.where(lane_head == h, prod, 0.0), 1, keepdims=True)
                    ds = r_.pst[l, head_rows(hf, h), rows].astype(F32) * (dp[k * R : (k + 1) * R] - delta)
                    r_.dss[h * R : (h + 1) * R] = ds.astype(BF16)
                part = dot(r_.dss[both], r_.kk[l, rows, lanes])
                parts += [part[0:R], part[R : 2 * R]]
            r_.dq[:, lanes] += by_head(parts)
            dk = dot(r_.qmT[hf], r_.dss[...]) * scale
            r_.dkv[pl.ds(pl.multiple_of(hf * 128, 128), 128)] = dk.astype(BF16)
            dv = dot(r_.dom[...].T, r_.pst[l, head_rows(hf, 0, HK), rows])
            r_.dkv[pl.ds(pl.multiple_of(D + hf * 128, 128), 128)] = dv.astype(BF16)
            between(i, hf)
            return carry

        lax.fori_loop(0, 2, heads, 0)
        dx = dot(r_.wqkv[l, :, D:], r_.dkv[...]).T
        r_.dxs[l, pl.ds(2 * half, 2)] = dx.astype(BF16).reshape(2, 2, R, D)

        @pl.when(i < NB - 1)
        def _():
            for low in range(2):
                zb = 2 * half + low
                send_rows(r_.dxs.at[l, zb, 1 - par], r_.rs1.at[l, zb], R,
                     r_.rsp_s.at[l, 2 * i + low], r_.rsp_r.at[l, 2 * i + low], nodes=partner)

        @pl.when(i == NB - 1)
        def _():
            near = z_to(1)
            send_rows(r_.dxs.at[l, z, 1 - par], r_.ro.at[l, 0], R, r_.ro_s.at[l, 0], r_.ro_r.at[l, 0], nodes=partner)
            send_rows(r_.dxs.at[l, near, par], r_.ro.at[l, 1], R, r_.ro_s.at[l, 1], r_.ro_r.at[l, 1], nodes=2 * near + par)
            send_rows(r_.dxs.at[l, near, 1 - par], r_.ro.at[l, 2], R, r_.ro_s.at[l, 2], r_.ro_r.at[l, 2],
                 nodes=2 * near + 1 - par)

        r_.gkv[...] += dot(r_.dkv[...], r_.xs[l, pl.ds(4 * half, 4)].reshape(W, D))

    def pass_on(l, i, t):
        zb = z_to(t)
        arrive(r_.rs1.at[l, zb], r_.rsp_r.at[l, 2 * i + zb % 2])
        both = r_.dxs[l, zb, par].astype(F32) + r_.rs1[l, zb].astype(F32)
        r_.cs[l, zb] = both.astype(BF16)
        send_rows(r_.cs.at[l, zb], r_.rs2.at[l, z], R, r_.rsc_s.at[l, t], r_.rsc_r.at[l, t], nodes=2 * zb + par)

    def back_convolution(l):
        s0, g0 = r_.gshift[l, 0:1], r_.ggain[l, 0:1]
        inv_den = 1.0 / (r_.den[l] + GATE_EPS)
        n0 = r_.z0[l] * r_.gain[l, 0:1] + r_.shift[l, 0:1]
        gy0 = r_.dmix[...] * silu_slope(n0)
        dm = r_.gain[l, 0:1] * r_.iv[l, 0:1] * (gy0 - s0 / total - r_.z0[l] * (g0 / total))
        dnum = dm * inv_den
        dden = -dnum * r_.num[l] * inv_den
        dnum_e = select_rows(r_.T[...], dnum)
        dden_e = select_rows(r_.T[...], dden)
        gate = r_.gate[l]
        dgp = (dnum_e * r_.bs[l].astype(F32) + dden_e) * gate * (1.0 - gate)
        r_.dce[...] = dgp.astype(BF16)
        dpb = select_rows(r_.ST[...], dnum_e * gate).astype(BF16)
        dpe = select_rows(r_.ST[...], dgp).astype(BF16)
        dpd = select_rows(r_.TT[...], dgp).astype(BF16)
        dmb = dm.astype(BF16)
        dxe = dot_nt(dpb, r_.wp[l, :, D : 2 * D]) + dot_nt(dpe, r_.wp[l, :, 3 * D :])
        r_.hs[l, 0] = dxe[R : R + 32].astype(BF16)
        r_.hs[l, 1] = dxe[R + 32 : R + 64].astype(BF16)
        send(r_.hs.at[l, 0], r_.hr.at[l, 1], r_.hal_s.at[l, 0], r_.hal_r.at[l, 0], nodes=prev)
        send(r_.hs.at[l, 1], r_.hr.at[l, 0], r_.hal_s.at[l, 1], r_.hal_r.at[l, 1], nodes=nxt)
        r_.dxo[...] += (
            dxe[0:R]
            + dot_nt(dmb, r_.wp[l, :, 0:D])
            + dot_nt(dpd, r_.wp[l, :, 2 * D : 3 * D])
        )
        r_.dproj[0, 0:R] = dmb
        r_.dproj[1] = dpb
        r_.dproj[2, 0:R] = dpd
        r_.dproj[3] = dpe

    def conv_weight_grads(l):
        at = 0
        for c in range(4):
            width = R if c % 2 == 0 else 256
            at = put(r_.gs_conv, l, at, dot(r_.xeT[:, 0:width], r_.dproj[c, 0:width]))
        put(r_.gs_conv, l, at, dot(r_.efT[...], r_.dce[...]))

    def back_input(l):
        dx = r_.dxo[...]
        dx = dx + r_.dxs[l, z, par].astype(F32)
        for slot in range(3):
            arrive(r_.ro.at[l, slot], r_.ro_r.at[l, slot])
            dx = dx + r_.ro[l, slot].astype(F32)
        for t in range(2, NZ):
            c = z_from(t)
            arrive(r_.rs2.at[l, c], r_.rsc_r.at[l, t])
            dx = dx + r_.rs2[l, c].astype(F32)
        arrive(r_.hr.at[l, 0], r_.hal_r.at[l, 1])
        arrive(r_.hr.at[l, 1], r_.hal_r.at[l, 0])
        back = jnp.concatenate(
            [r_.hr[l, 0].astype(F32)[0:24], r_.hr[l, 1].astype(F32)[0:24], jnp.zeros((16, D), F32)], 0
        )
        return dx + dot(r_.A[...], back.astype(BF16))

    r_.dy[...] = r_.cot[...].astype(F32)

    E1, C1, Q1 = BESIDE

    def steps(*pairs):
        return [functools.partial(reduce_step, g, k) for g, k in pairs]

    def backward(b, carry):
        l = L - 1 - b
        first, last = b == 0, b == L - 1
        k = 4 + 2 * b
        back_feed_forward(l, k)
        when(last, *steps((C1, 4), (Q1, 1), (E1, 5)))
        back_norms(l, k)
        when(first, *steps((E1, 0)))
        when(last, *steps((Q1, 2), (E1, 6), (C1, 5)))
        back_convolution(l)
        conv_weight_grads(l)
        when(first, *steps((E1, 1), (C1, 0)))
        when(last, *steps((Q1, 3), (C1, 6)))

        def between(i, hf):
            when(first & (i == 0) & (hf == 0), *steps((C1, 1)))
            when(first & (i == 0) & (hf == 1), *steps((E1, 2)))
            when(first & (i == 1) & (hf == 0), *steps((C1, 2)))
            when(first & (i == 1) & (hf == 1), *steps((E1, 3)))
            when(last & (i == 0) & (hf == 1), *steps((Q1, 4)))
            when(last & (i == 1) & (hf == 0), *steps((Q1, 5)))
            for t in range(2, NZ):
                when((i == 1) & (hf == 0), functools.partial(pass_on, l, 0, t))

        def block(i, carry):
            back_attention_block(l, i, between)
            return carry

        lax.fori_loop(0, NB, block, 0)
        dqb = (r_.dq[...] * scale).astype(BF16)
        r_.dxo[...] += dot_nt(dqb, r_.wqkv[l, :, 0:D])
        at = put(r_.gs_qkv, l, 0, dot(r_.xeT[:, 0:R], dqb))
        put(r_.gs_qkv, l, at, r_.gkv[...].T)
        when(first, *steps((Q1, 0)))

        @pl.when(first)
        def _():
            dx = back_input(l)
            r_.dy[...] = dx
            below = L - 2
            zero_row = jnp.zeros((1, D), F32)
            sync_start(5, pack(col_sum(dx), col_sum(dx * r_.z2[below]), zero_row, zero_row))
            for step in steps((C1, 3), (E1, 4)):
                step()
            s2, g2, _, _ = sync_finish(5, combine_sum)
            r_.gshift[below, 2:3] = s2
            r_.ggain[below, 2:3] = g2

        return carry

    lax.fori_loop(0, L, backward, 0)
    for step in steps((Q1, 6)):
        step()
    stores = [
        pltpu.make_async_copy(getattr(r_, f"gs_{name}").at[0], getattr(r_, f"{name}_out"), r_.store.at[2 + i])
        for i, name in enumerate(("early", "conv", "qkv"))
    ]
    for store in stores:
        store.start()
    r_.dy[...] = back_input(0)
    in_copy = pltpu.make_async_copy(r_.dy, r_.grad_in, r_.store.at[1])
    in_copy.start()
    for l in range(L):
        for k in range(3):
            r_.ggain_out[k, l : l + 1] = r_.ggain[l, k : k + 1]
            r_.gshift_out[k, l : l + 1] = r_.gshift[l, k : k + 1]
    for g in BESIDE:
        reduce_drain(g)
    for store in stores:
        store.wait()
    sent(r_.meta.at[0 : N - 1], r_.meta_s.at[0])
    for k in range(SYNCS):
        sent(r_.st1.at[k, 0 : M * N - 1], r_.st1_s.at[k])
    for l in range(L):
        for t in range(NZ):
            sent(r_.gb.at[l, 0], r_.agp_s.at[l, t])
            if t > 0:
                sent(r_.gb.at[l, 0], r_.agc_s.at[l, t])
            if t > 1:
                sent(r_.rs1.at[l, 0], r_.rsc_s.at[l, t])
        for slot in range(2 * (NB - 1)):
            sent(r_.rs1.at[l, 0], r_.rsp_s.at[l, slot])
        for slot in range(3):
            sent(r_.ro.at[l, 0], r_.ro_s.at[l, slot])
        for side in range(2):
            sent(r_.hs.at[l, 0], r_.hal_s.at[l, side])
    act_copy.wait()
    in_copy.wait()


def after_scratch(N, M):
    dma = lambda *shape: pltpu.SemaphoreType.DMA(shape)
    vm = lambda dtype, *shape: pltpu.VMEM(shape, dtype)
    return dict(
        gs_early=vm(BF16, 1, 2560, 128),
        gs_conv=vm(BF16, 1, 2560, 128),
        gs_qkv=vm(BF16, 1, 1536, 128),
        **group_scratch(N, M, AFTER),
        load=dma(3),
        ar_s=dma(len(GROUPS), 8),
        ar_r=dma(len(GROUPS), 8),
        ar_l=dma(len(GROUPS)),
    )


def after_kernel(N, M, names, *args):
    r_ = Refs()
    outs = tuple(f"gout{g}" for g in AFTER)
    for name, ref in zip(("early_h", "conv_h", "qkv_h") + outs + tuple(names), args, strict=True):
        setattr(r_, name, ref)
    me = lax.axis_index("nodes")
    _, send_rows, arrive, sent = senders(me + 1 - 2 * (me % 2))
    loads = [
        pltpu.make_async_copy(getattr(r_, f"{name}_h"), getattr(r_, f"gs_{name}").at[0], r_.load.at[i])
        for i, name in enumerate(("early", "conv", "qkv"))
    ]
    for load in loads:
        load.start()
    enter(N, M)
    for load in loads:
        load.wait()
    reduce_step, reduce_drain = reducers(r_, N, M, send_rows, arrive, sent)
    for step in range(2 * 4 + 1):
        for g in AFTER:
            reduce_step(g, step)
    for g in AFTER:
        reduce_drain(g)


def finish_kernel(act_h, gin_h, *refs):
    n = len(GROUPS)
    held, (ggain_h, gshift_h), refs = refs[:n], refs[n : n + 2], refs[n + 2 :]
    act_o, gin_o, proj_o, edge_o, qkv_o, out_o, up_o, down_o, ggain_o, gshift_o = refs[:10]
    summed, refs = refs[10 : 10 + n], refs[10 + n :]
    act, gin, proj, edge, qkv, out, up, down, in_sem, out_sem = refs
    loads = [
        pltpu.make_async_copy(src, dst, in_sem.at[i])
        for i, (src, dst) in enumerate(zip(held + (act_h, gin_h), summed + (act, gin), strict=True))
    ]
    for load in loads:
        load.start()
    ggain_o[...] = ggain_h[...]
    gshift_o[...] = gshift_h[...]
    stores = []

    def store(src, dst):
        copy = pltpu.make_async_copy(src, dst, out_sem.at[len(stores)])
        copy.start()
        stores.append(copy)

    def widen(dst, l, g, at, first=0, last=None):
        rows = dst.shape[1]
        for c in range(first, dst.shape[2] // 128 if last is None else last):
            dst[l, :, 128 * c : 128 * (c + 1)] = summed[g][at : at + rows].astype(F32)
            at += rows
        return at

    for g, (name, l, first, rows, _) in enumerate(GROUPS):
        loads[g].wait()
        if name == "early":
            at = widen(out, l, g, 0)
            store(out.at[l], out_o.at[l])
            at = widen(up, l, g, at)
            store(up.at[l], up_o.at[l])
            widen(down, l, g, at)
            store(down.at[l], down_o.at[l])
        elif name == "conv":
            at = widen(proj, l, g, 0)
            store(proj.at[l], proj_o.at[l])
            widen(edge, l, g, at)
            store(edge.at[l], edge_o.at[l])
        else:
            widen(qkv, l, g, 0, first // 256, (first + rows) // 256)
            if first + rows == 1536:
                store(qkv.at[l], qkv_o.at[l])
    for i, (src, dst) in enumerate(((act, act_o), (gin, gin_o))):
        loads[n + i].wait()
        store(src, dst)
    for copy in stores:
        copy.wait()


def fused_device(
    N, M, node_input, edge_feat, graph_ids, edge_src, edge_dst, halo_send, w_proj, w_edge, w_qkv,
    w_out, w_up, w_down, norm_gain, norm_shift, cotangent,
):
    R, D = node_input.shape
    E = edge_feat.shape[0]
    L = w_proj.shape[0]
    names = scratch_list(N, M, L, R, E)
    vmem = pl.BlockSpec(memory_space=pltpu.VMEM)
    hbm = pl.BlockSpec(memory_space=pltpu.HBM)
    shape = jax.ShapeDtypeStruct
    rows = shape((R, D), F32)
    norm = shape((3, L, D), F32)
    groups = [shape((rows_g, 128), BF16) for _, _, _, rows_g, _ in GROUPS]
    partial = [shape((count, 128), BF16) for count in (2560, 2560, 1536)]
    outs = pl.pallas_call(
        functools.partial(kernel, N, M, L, tuple(names)),
        out_shape=[rows, rows, *(groups[g] for g in BESIDE), *partial, norm, norm],
        in_specs=[hbm] + [vmem] * 4 + [hbm] * 7 + [vmem] * 2 + [hbm],
        out_specs=[hbm] * (2 + len(BESIDE) + 3) + [vmem] * 2,
        scratch_shapes=list(names.values()),
        compiler_params=pltpu.CompilerParams(
            collective_id=0, has_side_effects=True, vmem_limit_bytes=60 << 20
        ),
        name="layers",
    )(node_input, graph_ids, edge_src, edge_dst, halo_send, edge_feat, w_proj, w_edge, w_qkv, w_out, w_up,
      w_down, norm_gain.transpose(1, 0, 2), norm_shift.transpose(1, 0, 2), cotangent)
    act, gin, *summed, early, conv, qkv, ggain, gshift = outs
    names = after_scratch(N, M)
    summed += pl.pallas_call(
        functools.partial(after_kernel, N, M, tuple(names)),
        out_shape=[groups[g] for g in AFTER],
        in_specs=[hbm] * 3,
        out_specs=[hbm] * len(AFTER),
        scratch_shapes=list(names.values()),
        compiler_params=pltpu.CompilerParams(
            collective_id=1, has_side_effects=True, vmem_limit_bytes=60 << 20
        ),
        name="sums",
    )(early, conv, qkv)
    outs = (act, gin, *summed, ggain, gshift)
    weights = [shape(w.shape, F32) for w in (w_proj, w_edge, w_qkv, w_out, w_up, w_down)]
    results = pl.pallas_call(
        finish_kernel,
        out_shape=[rows, rows, *weights, norm, norm],
        in_specs=[hbm] * (2 + len(GROUPS)) + [vmem] * 2,
        out_specs=[hbm] * 8 + [vmem] * 2,
        scratch_shapes=[pltpu.VMEM(s.shape, s.dtype) for s in (*groups, rows, rows, *weights)]
        + [pltpu.SemaphoreType.DMA((len(GROUPS) + 2,)), pltpu.SemaphoreType.DMA((14,))],
        compiler_params=pltpu.CompilerParams(vmem_limit_bytes=60 << 20),
        name="gradients",
    )(*outs)
    ggain, gshift = results[8].transpose(1, 0, 2), results[9].transpose(1, 0, 2)
    return (*results[:8], ggain, gshift)


BLOCK_CAP = 2048


def extended_2(block, sides, width):
    for axis, dim in sides:
        count = lax.axis_size(axis)
        forward = [(i, i + 1) for i in range(count - 1)]
        forward.append((count - 1, 0))
        backward = [(target, source) for source, target in forward]
        low = lax.ppermute(
            lax.slice_in_dim(block, block.shape[dim] - width, None, axis=dim), axis, forward
        )
        high = lax.ppermute(lax.slice_in_dim(block, 0, width, axis=dim), axis, backward)
        block = jnp.concatenate([low, block, high], axis=dim)
    return block


def block_length(total_rows, upper_limit):
    for length in range(min(total_rows, upper_limit), 0, -1):
        if total_rows % length == 0:
            return length
    return 1


def outer_product(left, right):
    return lax.dot_general(
        left, right, (((0,), (0,)), ((), ())), preferred_element_type=jnp.float32
    )


def times_transposed(left, weight):
    return lax.dot_general(
        left, weight, (((1,), (1,)), ((), ())), preferred_element_type=jnp.float32
    )


def forward_product(left, weight):
    return jnp.dot(left, weight, preferred_element_type=jnp.float32)


def silu_slope_plain(inputs):
    logistic = jax.nn.sigmoid(inputs)
    return logistic * (1.0 + inputs * (1.0 - logistic))


def normalize(inputs, gain_row, shift_row, node_total):
    batch_mean = lax.psum(jnp.sum(inputs, 0), ("nodes", "rep")) / node_total
    centred = inputs - batch_mean
    batch_var = lax.psum(jnp.sum(centred * centred, 0), ("nodes", "rep")) / node_total
    inv_std = lax.rsqrt(batch_var + NORM_EPS)
    standard = (inputs - batch_mean) * inv_std
    return (standard * gain_row + shift_row, standard, inv_std)


def normalize_back(grad_out, standard, inv_std, gain_row, node_total):
    shift_grad, gain_grad = lax.psum(
        (jnp.sum(grad_out, 0), jnp.sum(grad_out * standard, 0)), ("nodes", "rep")
    )
    grad_in = (
        gain_row
        * inv_std
        * (grad_out - shift_grad / node_total - standard * gain_grad / node_total)
    )
    return (grad_in, gain_grad, shift_grad)


def exchange_sources(outgoing):
    halo_rows = outgoing.shape[0] // 2
    grown = extended_2(outgoing, (("nodes", 0),), halo_rows)
    return jnp.concatenate([grown[:halo_rows], grown[3 * halo_rows :]], 0)


def return_sources(incoming_grad):
    halo_rows = incoming_grad.shape[0] // 2
    grown = extended_2(incoming_grad.astype(jnp.bfloat16), (("nodes", 0),), halo_rows).astype(
        incoming_grad.dtype
    )
    return jnp.concatenate([grown[:halo_rows], grown[3 * halo_rows :]], 0)


def attend_forward(query_rows, key_rows, value_rows, local_graphs, group_graphs):
    row_count = query_rows.shape[0]
    score_scale = HEAD_DIM ** (-0.5)
    queries = query_rows.reshape(row_count, HEADS, HEAD_DIM)

    def add_piece(carried, kv_piece, first_row):
        key_piece, value_piece = kv_piece
        piece_rows = key_piece.shape[0]
        block_len = block_length(piece_rows, BLOCK_CAP)

        def add_block(block_state, block_index):
            row_max, row_sum, accumulated = block_state
            block_start = block_index * block_len
            key_block = lax.dynamic_slice_in_dim(key_piece, block_start, block_len, 0).reshape(
                block_len, HEADS, HEAD_DIM
            )
            value_block = lax.dynamic_slice_in_dim(value_piece, block_start, block_len, 0).reshape(
                block_len, HEADS, HEAD_DIM
            )
            key_graphs = lax.dynamic_slice_in_dim(
                group_graphs, first_row + block_start, block_len, 0
            )
            same_graph = (local_graphs[:, None] == key_graphs[None, :])[None]
            scores = (
                jnp.einsum("qhd,khd->hqk", queries, key_block, preferred_element_type=jnp.float32)
                * score_scale
            )
            scores = jnp.where(same_graph, scores, NEG)
            new_max = jnp.maximum(row_max, jnp.max(scores, 2))
            weights = jnp.where(same_graph, jnp.exp(scores - new_max[:, :, None]), 0.0)
            factor = jnp.exp(row_max - new_max)
            row_sum = row_sum * factor + jnp.sum(weights, 2)
            contrib = jnp.einsum(
                "hqk,khd->qhd",
                weights.astype(jnp.bfloat16),
                value_block,
                preferred_element_type=jnp.float32,
            )
            accumulated = accumulated * jnp.transpose(factor)[:, :, None] + contrib
            return ((new_max, row_sum, accumulated), None)

        carried, _ = lax.scan(add_block, carried, jnp.arange(piece_rows // block_len))
        return carried

    start_state = (
        jnp.full((HEADS, row_count), NEG, jnp.float32),
        jnp.zeros((HEADS, row_count), jnp.float32),
        jnp.zeros((row_count, HEADS, HEAD_DIM), jnp.float32),
    )
    row_max, row_sum, accumulated = add_piece(
        start_state,
        (
            lax.all_gather(key_rows, "nodes", axis=0, tiled=True),
            lax.all_gather(value_rows, "nodes", axis=0, tiled=True),
        ),
        jnp.int32(0),
    )
    attn_raw = accumulated / jnp.transpose(row_sum)[:, :, None]
    log_sum = row_max + jnp.log(row_sum)
    return (attn_raw, log_sum)


def attend_backward(
    query_rows, key_rows, value_rows, grad_low, attn_raw, log_sum, local_graphs, group_graphs
):
    row_count = query_rows.shape[0]
    model_width = HEADS * HEAD_DIM
    score_scale = HEAD_DIM ** (-0.5)
    queries = query_rows.reshape(row_count, HEADS, HEAD_DIM)
    grad_heads = grad_low.reshape(row_count, HEADS, HEAD_DIM)
    row_delta = jnp.einsum("qhd,qhd->hq", grad_heads.astype(jnp.float32), attn_raw)

    def score_block(key_block, value_block, key_graphs):
        same_graph = (local_graphs[:, None] == key_graphs[None, :])[None]
        scores = (
            jnp.einsum("qhd,khd->hqk", queries, key_block, preferred_element_type=jnp.float32)
            * score_scale
        )
        attn_weights = jnp.exp(jnp.where(same_graph, scores - log_sum[:, :, None], NEG))
        grad_weights = jnp.einsum(
            "qhd,khd->hqk", grad_heads, value_block, preferred_element_type=jnp.float32
        )
        grad_scores = (attn_weights * (grad_weights - row_delta[:, :, None])).astype(jnp.bfloat16)
        return (attn_weights, grad_scores)

    def key_terms(attn_weights, grad_scores, block_len):
        grad_keys = (
            jnp.einsum("hqk,qhd->khd", grad_scores, queries, preferred_element_type=jnp.float32)
            * score_scale
        )
        grad_values = jnp.einsum(
            "hqk,qhd->khd",
            attn_weights.astype(jnp.bfloat16),
            grad_heads,
            preferred_element_type=jnp.float32,
        )
        return jnp.concatenate(
            [
                grad_keys.reshape(block_len, model_width),
                grad_values.reshape(block_len, model_width),
            ],
            1,
        )

    def query_term(grad_scores, key_block):
        return (
            jnp.einsum("hqk,khd->qhd", grad_scores, key_block, preferred_element_type=jnp.float32)
            * score_scale
        )

    group_rows = group_graphs.shape[0]

    def add_piece(carried, kv_piece, first_row):
        key_piece, value_piece = kv_piece
        piece_rows = key_piece.shape[0]
        block_len = block_length(piece_rows, BLOCK_CAP)

        def add_block(block_state, block_index):
            grad_query, buffer = block_state
            block_start = block_index * block_len
            key_block = lax.dynamic_slice_in_dim(key_piece, block_start, block_len, 0).reshape(
                block_len, HEADS, HEAD_DIM
            )
            value_block = lax.dynamic_slice_in_dim(value_piece, block_start, block_len, 0).reshape(
                block_len, HEADS, HEAD_DIM
            )
            place = first_row + block_start
            key_graphs = lax.dynamic_slice_in_dim(group_graphs, place, block_len, 0)
            attn_weights, grad_scores = score_block(key_block, value_block, key_graphs)
            grad_query = grad_query + query_term(grad_scores, key_block)
            block_terms = key_terms(attn_weights, grad_scores, block_len)
            current = lax.dynamic_slice_in_dim(buffer, place, block_len, 0)
            buffer = lax.dynamic_update_slice_in_dim(buffer, current + block_terms, place, 0)
            return ((grad_query, buffer), None)

        carried, _ = lax.scan(add_block, carried, jnp.arange(piece_rows // block_len))
        return carried

    start_state = (
        jnp.zeros((row_count, HEADS, HEAD_DIM), jnp.float32),
        jnp.zeros((group_rows, 2 * model_width), jnp.float32),
    )
    grad_query, buffer = add_piece(
        start_state,
        (
            lax.all_gather(key_rows, "nodes", axis=0, tiled=True),
            lax.all_gather(value_rows, "nodes", axis=0, tiled=True),
        ),
        jnp.int32(0),
    )
    grad_kv = lax.psum_scatter(buffer, "nodes", scatter_dimension=0, tiled=True)
    return (
        grad_query.reshape(row_count, model_width),
        grad_kv[:, :model_width],
        grad_kv[:, model_width:],
    )


def layer_forward(
    hidden, params, edge_feat, edge_src, edge_dst, halo_send, local_graphs, group_graphs, node_total
):
    w_proj, w_edge, w_qkv, w_out, w_up, w_down, norm_gains, norm_shifts = params
    row_count, model_width = hidden.shape
    hidden_low = hidden.astype(jnp.bfloat16)
    projected = forward_product(hidden_low, w_proj)
    self_term = projected[:, :model_width]
    dest_term = projected[:, 2 * model_width : 3 * model_width]
    source_rows = jnp.concatenate(
        [projected[:, model_width : 2 * model_width], projected[:, 3 * model_width :]], 1
    ).astype(jnp.bfloat16)
    incoming = exchange_sources(source_rows[halo_send])
    extended = jnp.concatenate([source_rows, incoming], 0)
    edge_rows = extended[edge_src].astype(jnp.float32)
    source_b = edge_rows[:, :model_width]
    source_e = edge_rows[:, model_width:]
    edge_proj = forward_product(edge_feat, w_edge)
    gating = jax.nn.sigmoid(dest_term[edge_dst] + source_e + edge_proj)
    numerator = jax.ops.segment_sum(gating * source_b, edge_dst, row_count)
    denominator = jax.ops.segment_sum(gating, edge_dst, row_count)
    message = self_term + numerator / (denominator + GATE_EPS)
    normed_one, standard_one, inv_one = normalize(
        message, norm_gains[0], norm_shifts[0], node_total
    )
    local_out = hidden + jax.nn.silu(normed_one)
    qkv_low = forward_product(hidden_low, w_qkv).astype(jnp.bfloat16)
    query_rows = qkv_low[:, :model_width]
    key_rows = qkv_low[:, model_width : 2 * model_width]
    value_rows = qkv_low[:, 2 * model_width :]
    attn_raw, log_sum = attend_forward(query_rows, key_rows, value_rows, local_graphs, group_graphs)
    attn_low = attn_raw.reshape(row_count, model_width).astype(jnp.bfloat16)
    attn_proj = forward_product(attn_low, w_out)
    normed_two, standard_two, inv_two = normalize(
        hidden + attn_proj, norm_gains[1], norm_shifts[1], node_total
    )
    mixed = local_out + normed_two
    mixed_low = mixed.astype(jnp.bfloat16)
    up_proj = forward_product(mixed_low, w_up)
    activated = jax.nn.silu(up_proj).astype(jnp.bfloat16)
    down_proj = forward_product(activated, w_down)
    normed_three, standard_three, inv_three = normalize(
        mixed + down_proj, norm_gains[2], norm_shifts[2], node_total
    )
    saved = (
        hidden_low,
        source_b,
        gating,
        numerator,
        denominator,
        normed_one,
        standard_one,
        inv_one,
        query_rows,
        key_rows,
        value_rows,
        attn_raw,
        log_sum,
        attn_low,
        standard_two,
        inv_two,
        mixed_low,
        up_proj,
        activated,
        standard_three,
        inv_three,
    )
    return (normed_three, saved)


def layer_backward(
    grad_out,
    params,
    saved,
    edge_feat,
    edge_src,
    edge_dst,
    halo_send,
    local_graphs,
    group_graphs,
    node_total,
):
    w_proj, w_edge, w_qkv, w_out, w_up, w_down, norm_gains, norm_shifts = params
    (
        hidden_low,
        source_b,
        gating,
        numerator,
        denominator,
        normed_one,
        standard_one,
        inv_one,
        query_rows,
        key_rows,
        value_rows,
        attn_raw,
        log_sum,
        attn_low,
        standard_two,
        inv_two,
        mixed_low,
        up_proj,
        activated,
        standard_three,
        inv_three,
    ) = saved
    row_count, model_width = grad_out.shape
    grad_three, gain_three, shift_three = normalize_back(
        grad_out, standard_three, inv_three, norm_gains[2], node_total
    )
    down_grad = grad_three.astype(jnp.bfloat16)
    grad_w_down = outer_product(activated, down_grad)
    up_grad = (times_transposed(down_grad, w_down) * silu_slope_plain(up_proj)).astype(jnp.bfloat16)
    grad_w_up = outer_product(mixed_low, up_grad)
    grad_mixed = grad_three + times_transposed(up_grad, w_up)
    grad_two, gain_two, shift_two = normalize_back(
        grad_mixed, standard_two, inv_two, norm_gains[1], node_total
    )
    out_grad = grad_two.astype(jnp.bfloat16)
    grad_w_out = outer_product(attn_low, out_grad)
    attn_grad = times_transposed(out_grad, w_out).astype(jnp.bfloat16)
    grad_query, grad_key, grad_value = attend_backward(
        query_rows, key_rows, value_rows, attn_grad, attn_raw, log_sum, local_graphs, group_graphs
    )
    qkv_grad = jnp.concatenate([grad_query, grad_key, grad_value], 1).astype(jnp.bfloat16)
    grad_w_qkv = outer_product(hidden_low, qkv_grad)
    grad_message, gain_one, shift_one = normalize_back(
        grad_mixed * silu_slope_plain(normed_one), standard_one, inv_one, norm_gains[0], node_total
    )
    shifted = denominator + GATE_EPS
    grad_numer = grad_message / shifted
    grad_denom = -grad_message * numerator / (shifted * shifted)
    numer_edge = grad_numer[edge_dst]
    grad_gate = numer_edge * source_b + grad_denom[edge_dst]
    grad_pre_edge = grad_gate * gating * (1.0 - gating)
    edge_grad = grad_pre_edge.astype(jnp.bfloat16)
    grad_w_edge = outer_product(edge_feat, edge_grad)
    grad_dest = jax.ops.segment_sum(grad_pre_edge, edge_dst, row_count)
    grad_extended = jax.ops.segment_sum(
        jnp.concatenate([numer_edge * gating, grad_pre_edge], 1),
        edge_src,
        row_count + halo_send.shape[0],
    )
    returned = return_sources(grad_extended[row_count:])
    grad_source = grad_extended[:row_count].at[halo_send].add(returned)
    proj_grad = jnp.concatenate(
        [grad_message, grad_source[:, :model_width], grad_dest, grad_source[:, model_width:]], 1
    ).astype(jnp.bfloat16)
    grad_w_proj = outer_product(hidden_low, proj_grad)
    grad_hidden = (
        grad_mixed
        + grad_two
        + times_transposed(proj_grad, w_proj)
        + times_transposed(qkv_grad, w_qkv)
    )
    weight_grads = (grad_w_proj, grad_w_edge, grad_w_qkv, grad_w_out, grad_w_up, grad_w_down)
    return (
        grad_hidden,
        weight_grads,
        jnp.stack([gain_one, gain_two, gain_three]),
        jnp.stack([shift_one, shift_two, shift_three]),
    )


def per_device(
    node_input,
    edge_feat,
    graph_ids,
    edge_src,
    edge_dst,
    halo_send,
    w_proj,
    w_edge,
    w_qkv,
    w_out,
    w_up,
    w_down,
    norm_gain,
    norm_shift,
    cotangent,
):
    group_graphs = lax.all_gather(graph_ids, "nodes", axis=0, tiled=True)
    node_total = node_input.shape[0] * lax.axis_size("nodes") * lax.axis_size("rep")
    layer_count = w_proj.shape[0]
    layer_params = [
        (
            w_proj[layer_index],
            w_edge[layer_index],
            w_qkv[layer_index],
            w_out[layer_index],
            w_up[layer_index],
            w_down[layer_index],
            norm_gain[layer_index],
            norm_shift[layer_index],
        )
        for layer_index in range(layer_count)
    ]
    hidden = node_input.astype(jnp.float32)
    saved_all = []
    for layer_index in range(layer_count):
        hidden, saved = layer_forward(
            hidden,
            layer_params[layer_index],
            edge_feat,
            edge_src,
            edge_dst,
            halo_send,
            graph_ids,
            group_graphs,
            node_total,
        )
        saved_all.append(saved)
    grad_hidden = cotangent.astype(jnp.float32)
    weight_parts = [None] * layer_count
    gain_parts = [None] * layer_count
    shift_parts = [None] * layer_count
    for layer_index in range(layer_count - 1, -1, -1):
        (
            grad_hidden,
            weight_parts[layer_index],
            gain_parts[layer_index],
            shift_parts[layer_index],
        ) = layer_backward(
            grad_hidden,
            layer_params[layer_index],
            saved_all[layer_index],
            edge_feat,
            edge_src,
            edge_dst,
            halo_send,
            graph_ids,
            group_graphs,
            node_total,
        )
    proj_local = jnp.stack([weight_parts[layer_index][0] for layer_index in range(layer_count)])
    edge_local = jnp.stack([weight_parts[layer_index][1] for layer_index in range(layer_count)])
    qkv_local = jnp.stack([weight_parts[layer_index][2] for layer_index in range(layer_count)])
    out_local = jnp.stack([weight_parts[layer_index][3] for layer_index in range(layer_count)])
    up_local = jnp.stack([weight_parts[layer_index][4] for layer_index in range(layer_count)])
    down_local = jnp.stack([weight_parts[layer_index][5] for layer_index in range(layer_count)])
    grad_proj, grad_edge, grad_qkv, grad_out, grad_up, grad_down = lax.psum(
        (proj_local, edge_local, qkv_local, out_local, up_local, down_local), ("nodes", "rep")
    )
    return (
        hidden,
        grad_hidden,
        grad_proj,
        grad_edge,
        grad_qkv,
        grad_out,
        grad_up,
        grad_down,
        jnp.stack(gain_parts),
        jnp.stack(shift_parts),
    )


def solution(mesh):
    in_specs = (
        P(("rep", "nodes"), None),
        P(("rep", "nodes"), None),
        P(("rep", "nodes")),
        P(("rep", "nodes")),
        P(("rep", "nodes")),
        P(("rep", "nodes")),
        P(),
        P(),
        P(),
        P(),
        P(),
        P(),
        P(),
        P(),
        P(("rep", "nodes"), None),
    )
    out_specs = (
        P(("rep", "nodes"), None),
        P(("rep", "nodes"), None),
        P(),
        P(),
        P(),
        P(),
        P(),
        P(),
        P(),
        P(),
    )
    N, M = mesh.shape["nodes"], mesh.shape["rep"]
    fused = N in (4, 8) and M % 2 == 0 and 512 % (16 * N * M) == 0
    return jax.shard_map(
        functools.partial(fused_device, N, M) if fused else per_device,
        mesh=mesh, in_specs=in_specs, out_specs=out_specs, check_vma=False,
    )
```

```python
import functools
import math

import jax
import jax.numpy as jnp
from jax import lax
from jax.experimental import pallas as pl
from jax.experimental.pallas import tpu as pltpu
from jax.sharding import PartitionSpec as P

HEADS = 8
HEAD_DIM = 32
NEG = -1e30
NORM_EPS = 1e-05
GATE_EPS = 1e-06
F32, BF16, I32 = jnp.float32, jnp.bfloat16, jnp.int32
MESH = pl.DeviceIdType.MESH
SYNCS = 12
GROUPS = (
    ("early", 1, 0, 2560, ("core", "y", "nodes")),
    ("conv", 1, 0, 2560, ("core", "x", "y", "z")),
    ("qkv", 1, 0, 1536, ("core", "y", "nodes")),
    ("early", 0, 0, 2560, ("core", "x", "y", "z")),
    ("conv", 0, 0, 2560, ("core", "y", "nodes")),
    ("qkv", 0, 0, 1536, ("rep", "nodes")),
)


def dot(left, right):
    return lax.dot_general(
        left, right, (((1,), (0,)), ((), ())), preferred_element_type=F32
    )


def dot_nt(left, right):
    return lax.dot_general(
        left, right, (((1,), (1,)), ((), ())), preferred_element_type=F32
    )


def dot_tn(left, right):
    return lax.dot_general(
        left, right, (((0,), (0,)), ((), ())), preferred_element_type=F32
    )


def split(value):
    high = value.astype(BF16)
    return high, (value - high.astype(F32)).astype(BF16)


def select_rows(onehot, value):
    high, low = split(value)
    return dot(onehot, high) + dot(onehot, low)


def sigmoid(value):
    return 1.0 / (1.0 + jnp.exp(-value))


def silu_slope(value):
    logistic = sigmoid(value)
    return logistic * (1.0 + value * (1.0 - logistic))


def col_sum(value):
    return jnp.sum(value, axis=0, keepdims=True)


def pack(first, second):
    return jnp.concatenate([first[:, :128], first[:, 128:], second[:, :128], second[:, 128:]], 0)


def unpack(tile):
    return [jnp.concatenate([tile[i : i + 1], tile[i + 1 : i + 2]], 1) for i in (0, 2)]


def combine_moments(tiles, count):
    mean = jnp.mean(tiles[:, 0:2], 0)
    off = tiles[:, 0:2] - mean
    return jnp.concatenate([mean, jnp.sum(tiles[:, 2:4] + count * off * off, 0)], 0)


class Refs:
    pass


def axis_sizes(N, M):
    return dict(core=2, y=M // 2, x=2, z=N // 2, rep=M, nodes=N)


def scratch_list(N, M, L, R, E):
    NZ, NB, G = N // 2, N // 4, N * R
    D, FF, W, HH = 256, 512, 4 * R, HEADS // 2 * R
    dma = lambda *shape: pltpu.SemaphoreType.DMA(shape)
    vm = lambda dtype, *shape: pltpu.VMEM(shape, dtype)
    names = dict(
        gb=vm(BF16, L, N, R, D),
        xs=vm(BF16, L, N, R, D),
        meta=vm(I32, N, 8, 256),
        ef=vm(BF16, E, D),
        cot=vm(BF16, R, D),
        wp=vm(BF16, L, D, 4 * D),
        we=vm(BF16, L, D, D),
        wqkv=vm(BF16, L, D, 3 * D),
        wo=vm(BF16, L, D, D),
        wu=vm(BF16, L, D, FF),
        wd=vm(BF16, L, FF, D),
        st1=vm(F32, SYNCS, M * N, 4, 128),
        gain=vm(F32, L, 8, D),
        shift=vm(F32, L, 8, D),
        ggain=vm(F32, L, 8, D),
        gshift=vm(F32, L, 8, D),
        iv=vm(F32, L, 8, D),
        moff=vm(F32, N, 8, D),
        move=vm(F32, 8, D),
        T=vm(BF16, E, R),
        TT=vm(BF16, R, E),
        S=vm(BF16, E, 256),
        ST=vm(BF16, 256, E),
        efT=vm(BF16, D, E),
        HP=vm(BF16, 32, R),
        HN=vm(BF16, 32, R),
        A=vm(BF16, R, 64),
        bias=vm(F32, R, G),
        ce=vm(F32, L, E, D),
        xf=vm(F32, L + 1, R, D),
        xe=vm(BF16, L, 256, D),
        xeT=vm(BF16, D, 256),
        gate=vm(F32, L, E, D),
        bs=vm(BF16, L, E, D),
        num=vm(F32, L, R, D),
        den=vm(F32, L, R, D),
        z0=vm(F32, L, R, D),
        z1=vm(F32, L, R, D),
        z2=vm(F32, L, R, D),
        kk=vm(BF16, L, G, D),
        vv=vm(BF16, L, G, D),
        kT=vm(BF16, D, G),
        vT=vm(BF16, D, G),
        od=vm(F32, NB, R, D),
        md=vm(F32, NB, R, D),
        ld=vm(F32, NB, R, D),
        rb=vm(F32, L, NB, R, D),
        pst=vm(BF16, L, HEADS * R, G),
        oraw=vm(F32, L, R, D),
        ob=vm(BF16, L, R, D),
        mb=vm(BF16, L, R, D),
        u=vm(F32, L, R, FF),
        g=vm(BF16, L, R, FF),
        dy=vm(F32, R, D),
        dmix=vm(F32, R, D),
        gy0=vm(F32, R, D),
        local=vm(F32, R, D),
        dxo=vm(F32, R, D),
        dob=vm(F32, R, D),
        dq=vm(F32, R, D),
        qm=vm(BF16, L, 2, HH, 128),
        qmT=vm(BF16, 2, 128, HH),
        dom=vm(BF16, HH, 128),
        dss=vm(BF16, HH, W),
        dkv=vm(BF16, 2 * D, W),
        gkv=vm(F32, 2 * D, D),
        dce=vm(BF16, E, D),
        dproj=vm(BF16, 4, 256, D),
        dxs=vm(BF16, L, NZ, 2, R, D),
        rs1=vm(BF16, L, NZ, R, D),
        cs=vm(BF16, L, NZ, R, D),
        rs2=vm(BF16, L, NZ, R, D),
        ro=vm(BF16, L, 3, R, D),
        hs=vm(BF16, L, 2, 32, D),
        hr=vm(BF16, L, 2, 32, D),
    )
    names.update(
        gs_early=vm(BF16, L, 2560, 128),
        gs_conv=vm(BF16, L, 2560, 128),
        gs_qkv=vm(BF16, L, 1536, 128),
    )
    sizes = axis_sizes(N, M)
    for g, (_, _, _, rows, stages) in enumerate(GROUPS):
        names[f"go{g}"] = vm(BF16, rows, 128)
        left = rows
        for k, axis in enumerate(stages):
            left //= sizes[axis]
            names[f"ga{g}_{k}"] = vm(BF16, sizes[axis] - 1, left, 128)
            if k < len(stages) - 1:
                names[f"gh{g}_{k}"] = vm(BF16, left, 128)
    names.update(
        ar_s=dma(len(GROUPS), 8),
        ar_r=dma(len(GROUPS), 8),
        ar_l=dma(len(GROUPS)),
        load=dma(10),
        store=dma(2),
        meta_s=dma(1),
        meta_r=dma(1),
        st1_s=dma(SYNCS),
        st1_r=dma(SYNCS),
        agc_s=dma(L, NZ),
        agc_r=dma(L, NZ),
        agp_s=dma(L, NZ),
        agp_r=dma(L, NZ),
        rsp_s=dma(L, NZ),
        rsp_r=dma(L, NZ),
        ro_s=dma(L, 3),
        ro_r=dma(L, 3),
        rsc_s=dma(L, NZ),
        rsc_r=dma(L, NZ),
        hal_s=dma(L, 2),
        hal_r=dma(L, 2),
    )
    return names


IN_NAMES = (
    "x_in", "ids", "edge_src", "edge_dst", "halo", "ef_h", "wp_h", "we_h", "wqkv_h", "wo_h", "wu_h", "wd_h",
    "gain_in", "shift_in", "cot_h",
)
OUT_NAMES = ("out_act", "grad_in", *(f"gout{g}" for g in range(len(GROUPS))), "ggain_out", "gshift_out")


def kernel(N, M, L, names, *args):
    r_ = Refs()
    for name, ref in zip(IN_NAMES + OUT_NAMES + tuple(names), args, strict=True):
        setattr(r_, name, ref)
    R, D = r_.x_in.shape
    E = r_.ef.shape[0]
    NZ, NB, G, W = N // 2, N // 4, N * R, 4 * R
    HK = HEADS // 2
    total = float(N * M * R)
    scale = HEAD_DIM ** -0.5
    me = lax.axis_index("nodes")
    rep = lax.axis_index("rep")
    z = me // 2
    par = me % 2
    partner = 2 * z + (1 - par)
    prev = (me + N - 1) % N
    nxt = (me + 1) % N
    zh, zl = z // 2, z % 2
    z_to = lambda t: 2 * ((zh + t // 2) % NB) + (zl + t % 2) % 2
    z_from = lambda t: 2 * ((zh + NB - t // 2) % NB) + (zl + t % 2) % 2

    def remote(src, dst, s_sem, r_sem, **where):
        return pltpu.make_async_remote_copy(
            src_ref=src, dst_ref=dst, send_sem=s_sem, recv_sem=r_sem,
            device_id=where, device_id_type=MESH,
        )

    def send(src, dst, s_sem, r_sem, **where):
        remote(src, dst, s_sem, r_sem, **where).start()

    def send_rows(src, dst, rows, s_sem, r_sem, **where):
        pieces = next(p for p in range(1, rows) if rows % (16 * p) == 0 and rows // p <= 128)
        for at in range(0, rows, rows // pieces):
            cut = pl.ds(at, rows // pieces)
            send(src.at[cut], dst.at[cut], s_sem, r_sem, **where)

    def arrive(dst, r_sem):
        remote(dst, dst, r_sem, r_sem, nodes=partner).wait_recv()

    def sent(src, s_sem):
        remote(src, src, s_sem, s_sem, nodes=partner).wait_send()

    def when(condition, *acts):
        @pl.when(condition)
        def _():
            for act in acts:
                act()

    loads = [
        pltpu.make_async_copy(getattr(r_, f"{name}_h"), getattr(r_, name), r_.load.at[i])
        for i, name in enumerate(("ef", "we", "wqkv", "wp", "wo", "wu", "wd", "cot"))
    ]
    own_rows = pltpu.make_async_copy(r_.x_in, r_.gb.at[0, me], r_.load.at[8])
    own_rows.start()
    for load in loads:
        load.start()

    barrier = pltpu.get_barrier_semaphore()
    for dr in range(M):
        for d in range(N):
            if dr + d > 0:
                pl.semaphore_signal(barrier, inc=1, device_id={"rep": (rep + dr) % M, "nodes": (me + d) % N},
                                    device_id_type=MESH)
    pl.semaphore_wait(barrier, M * N - 1)

    def gather_start(l):
        mine = r_.gb.at[l, me]
        send_rows(mine, mine, R, r_.agp_s.at[l, 0], r_.agp_r.at[l, 0], nodes=partner)
        send_rows(mine, mine, R, r_.agc_s.at[l, 1], r_.agc_r.at[l, 1], nodes=2 * z_to(1) + par)
        send_rows(mine, mine, R, r_.agp_s.at[l, 1], r_.agp_r.at[l, 1], nodes=2 * z_to(1) + 1 - par)
        for t in range(2, NZ):
            send_rows(mine, mine, R, r_.agc_s.at[l, t], r_.agc_r.at[l, t], nodes=2 * z_to(t) + par)

    def gather_pass(l, t):
        piece = r_.gb.at[l, 2 * z_from(t) + par]
        arrive(piece, r_.agc_r.at[l, t])
        send_rows(piece, piece, R, r_.agp_s.at[l, t], r_.agp_r.at[l, t], nodes=partner)

    def gather_take(l, t):
        arrive(r_.gb.at[l, 2 * z_from(t) + 1 - par], r_.agp_r.at[l, t])

    def sync_start(k, first, second):
        mine = rep * N + me
        r_.st1[k, mine] = pack(first, second)
        for dr in range(M):
            for d in range(N):
                if dr + d > 0:
                    send(r_.st1.at[k, mine], r_.st1.at[k, mine], r_.st1_s.at[k], r_.st1_r.at[k],
                         rep=(rep + dr) % M, nodes=(me + d) % N)

    def sync_wait(k):
        arrive(r_.st1.at[k, 0 : M * N - 1], r_.st1_r.at[k])

    def sync_moments(k):
        sync_wait(k)
        return unpack(combine_moments(r_.st1[k], float(R)))

    def sync_sums(k):
        sync_wait(k)
        return unpack(jnp.sum(r_.st1[k], 0))

    sizes = axis_sizes(N, M)
    core, row = rep % 2, rep // 2
    places = dict(
        core=(core, lambda t: dict(rep=2 * row + t)),
        y=(row, lambda t: dict(rep=2 * t + core)),
        x=(par, lambda t: dict(nodes=2 * z + t)),
        z=(z, lambda t: dict(nodes=2 * t + par)),
        rep=(rep, lambda t: dict(rep=t)),
        nodes=(me, lambda t: dict(nodes=t)),
    )

    def reduce_step(g, step):
        name, layer, first, rows, stages = GROUPS[g]
        K = len(stages)
        gs, out = getattr(r_, f"gs_{name}").at[layer, first : first + rows], getattr(r_, f"go{g}")
        count, offset = [rows], [0]
        for axis in stages:
            count.append(count[-1] // sizes[axis])
            offset.append(offset[-1] + places[axis][0] * count[-1])
        take = lambda start, size: pl.ds(pl.multiple_of(start, 16), size)
        if 1 <= step <= K:
            k = step - 1
            got = getattr(r_, f"ga{g}_{k}")
            arrive(got, r_.ar_r.at[g, k])
            held = gs if k == 0 else getattr(r_, f"gh{g}_{k - 1}")
            index = places[stages[k]][0]
            acc = held[take(index * count[k + 1], count[k + 1])].astype(F32)
            for slot in range(sizes[stages[k]] - 1):
                acc = acc + got[slot].astype(F32)
            if step < K:
                getattr(r_, f"gh{g}_{k}")[...] = acc.astype(BF16)
            else:
                out[take(offset[K], count[K])] = acc.astype(BF16)
        elif step > K:
            k = 2 * K - step
            arrive(out.at[0 : (sizes[stages[k]] - 1) * count[k + 1]], r_.ar_r.at[g, step - 1])
        if step < K:
            held = gs if step == 0 else getattr(r_, f"gh{g}_{step - 1}")
            index, device = places[stages[step]]
            size = sizes[stages[step]]
            for d in range(1, size):
                to = (index + d) % size
                send_rows(held.at[take(to * count[step + 1], count[step + 1])], getattr(r_, f"ga{g}_{step}").at[d - 1],
                     count[step + 1], r_.ar_s.at[g, step], r_.ar_r.at[g, step], **device(to))
        elif step < 2 * K:
            k = 2 * K - 1 - step
            index, device = places[stages[k]]
            size = sizes[stages[k]]
            here = out.at[take(offset[k + 1], count[k + 1])]
            for d in range(1, size):
                send_rows(here, here, count[k + 1], r_.ar_s.at[g, step], r_.ar_r.at[g, step],
                          **device((index + d) % size))
        else:
            pltpu.make_async_copy(out, getattr(r_, f"gout{g}"), r_.ar_l.at[g]).start()

    def reduce_drain(g):
        _, _, _, rows, stages = GROUPS[g]
        K, left = len(stages), rows
        out = getattr(r_, f"go{g}")
        for k, axis in enumerate(stages):
            left //= sizes[axis]
            for step in (k, 2 * K - 1 - k):
                sent(out.at[0 : (sizes[axis] - 1) * left], r_.ar_s.at[g, step])
        pltpu.make_async_copy(out, getattr(r_, f"gout{g}"), r_.ar_l.at[g]).wait()

    def put(buf, l, at, value):
        rows = value.shape[0]
        for c in range(value.shape[1] // 128):
            buf[l, at : at + rows] = value[:, 128 * c : 128 * (c + 1)].astype(BF16)
            at += rows
        return at

    lane_head = lax.broadcasted_iota(I32, (R, 128), 1) // HEAD_DIM

    def by_head(parts):
        out = parts[0]
        for k in range(1, HK):
            out = jnp.where(lane_head == k, parts[k], out)
        return out

    r_.meta[me] = jnp.full((8, 256), -1, I32)
    r_.meta[me, 0:1, 0:R] = r_.ids[...].reshape(1, R)
    r_.meta[me, 1:2, 0:48] = r_.halo[...].reshape(1, 48)
    for d in range(1, N):
        send(r_.meta.at[me], r_.meta.at[me], r_.meta_s.at[0], r_.meta_r.at[0], nodes=(me + d) % N)
    own_rows.wait()
    gather_start(0)

    src_row = r_.edge_src[...].reshape(1, E)
    src_row = jnp.where(src_row < R + 24, src_row, src_row + 8)
    dst_row = r_.edge_dst[...].reshape(1, E)
    src_col = jnp.broadcast_to(src_row, (128, E)).T[:, 0:1]
    dst_col = jnp.broadcast_to(dst_row, (128, E)).T[:, 0:1]
    as_mask = lambda cond: cond.astype(F32).astype(BF16)
    r_.T[...] = as_mask(dst_col == lax.broadcasted_iota(I32, (E, R), 1))
    r_.TT[...] = as_mask(dst_row == lax.broadcasted_iota(I32, (R, E), 0))
    r_.S[...] = as_mask(src_col == lax.broadcasted_iota(I32, (E, 256), 1))
    r_.ST[...] = as_mask(src_row == lax.broadcasted_iota(I32, (256, E), 0))
    loads[0].wait()
    r_.efT[...] = r_.ef[...].T
    loads[1].wait()
    for l in range(L):
        r_.ce[l] = dot(r_.ef[...], r_.we[l])
        for k in range(3):
            r_.gain[l, k : k + 1] = r_.gain_in[k, l : l + 1]
            r_.shift[l, k : k + 1] = r_.shift_in[k, l : l + 1]
    r_.xf[0] = r_.gb[0, me].astype(F32)
    r_.moff[...] = jnp.zeros((N, 8, D), F32)
    r_.move[0:1] = jnp.ones((1, D), F32)
    r_.move[1:2] = jnp.zeros((1, D), F32)
    for load in loads[2:]:
        load.wait()

    arrive(r_.meta.at[0 : N - 1], r_.meta_r.at[0])
    id_col = jnp.broadcast_to(r_.meta[me][0:1, 0:R], (128, R)).T[:, 0:1]
    id_row = jnp.concatenate([r_.meta[j][0:1, 0:R] for j in range(N)], 1)
    r_.bias[...] = jnp.where(id_col == id_row, 0.0, NEG)

    def halo_onehot(device, start):
        col = jnp.broadcast_to(r_.meta[device][1:2, 0:128], (128, 128)).T[start : start + 24, 0:1]
        hot = (col == lax.broadcasted_iota(I32, (24, R), 1)).astype(F32)
        return jnp.concatenate([hot, jnp.zeros((8, R), F32)], 0).astype(BF16)

    r_.HP[...] = halo_onehot(prev, 24)
    r_.HN[...] = halo_onehot(nxt, 0)
    r_.A[...] = as_mask(r_.meta[me][1:2, 0:64] == lax.broadcasted_iota(I32, (R, 64), 0))

    factor_exp = scale * math.log2(math.e)

    def prepare_queries(l):
        q = dot(r_.xs[l, me], r_.wqkv[l, :, :D]).astype(BF16).astype(F32)
        for hf in range(2):
            for k in range(HK):
                part = jnp.where(lane_head == k, q[:, 128 * hf : 128 * (hf + 1)], 0.0)
                r_.qm[l, hf, k * R : (k + 1) * R] = part.astype(BF16)

    def head_rows(hf, k, count=1):
        return pl.ds(pl.multiple_of((hf * HK + k) * R, 64), count * R)

    def lane_half(hf):
        return pl.ds(pl.multiple_of(hf * 128, 128), 128)

    def attention_block(l, i, middle):
        half = (zh + NB - i) % NB
        rows = pl.ds(pl.multiple_of(half * W, 128), W)
        x = r_.xs[l, pl.ds(4 * half, 4)].reshape(W, D)
        key = dot(x, r_.wqkv[l, :, D : 2 * D]).astype(BF16)
        r_.kk[l, rows] = key
        r_.kT[:, rows] = key.T
        r_.vv[l, rows] = dot(x, r_.wqkv[l, :, 2 * D :]).astype(BF16)

        def heads(hf, carry):
            lanes = lane_half(hf)
            tops, sums, outs = [], [], []
            for c in range(HK // 2):
                scores = dot(r_.qm[l, hf, 2 * c * R : 2 * (c + 1) * R], r_.kT[lanes, rows])
                for k in range(2):
                    s = scores[k * R : (k + 1) * R] + r_.bias[:, rows]
                    top = jnp.max(s, 1, keepdims=True)
                    e = jnp.exp2((s - top) * factor_exp)
                    tops.append(top)
                    sums.append(jnp.sum(e, 1, keepdims=True))
                    r_.pst[l, head_rows(hf, 2 * c + k), rows] = e.astype(BF16)
                o = dot(r_.pst[l, head_rows(hf, 2 * c, 2), rows], r_.vv[l, rows, lanes])
                outs += [o[0:R], o[R : 2 * R]]
            r_.md[i, :, lanes] = by_head([jnp.broadcast_to(v, (R, 128)) for v in tops])
            r_.ld[i, :, lanes] = by_head([jnp.broadcast_to(v, (R, 128)) for v in sums])
            r_.od[i, :, lanes] = by_head(outs)
            middle(i, hf)
            return carry

        lax.fori_loop(0, 2, heads, 0)

    def attention_end(l):
        top = r_.md[0]
        for i in range(1, NB):
            top = jnp.maximum(top, r_.md[i])
        factors = [jnp.exp2((r_.md[i] - top) * factor_exp) for i in range(NB)]
        inv = 1.0 / sum(factors[i] * r_.ld[i] for i in range(NB))
        o = jnp.zeros((R, D), F32)
        for i in range(NB):
            r_.rb[l, i] = factors[i] * inv
            o = o + factors[i] * inv * r_.od[i]
        r_.oraw[l] = o
        ob = o.astype(BF16)
        r_.ob[l] = ob
        t1 = r_.xf[l] + dot(ob, r_.wo[l])
        r_.z1[l] = t1
        mean1 = col_sum(t1) / R
        return mean1, col_sum((t1 - mean1) * (t1 - mean1))

    def convolution(l):
        xs = r_.xs
        xb = xs[l, me]
        r_.xe[l, 0:R] = xb
        r_.xe[l, R : R + 32] = dot(r_.HP[...], xs[l, prev]).astype(BF16)
        r_.xe[l, R + 32 : R + 64] = dot(r_.HN[...], xs[l, nxt]).astype(BF16)
        xe = r_.xe[l]
        tab_b = dot(xe, r_.wp[l, :, D : 2 * D]).astype(BF16)
        tab_e = dot(xe, r_.wp[l, :, 3 * D :]).astype(BF16)
        pa = dot(xb, r_.wp[l, :, 0:D])
        pd = dot(xb, r_.wp[l, :, 2 * D : 3 * D])
        bs = dot(r_.S[...], tab_b)
        r_.bs[l] = bs.astype(BF16)
        gate = sigmoid(select_rows(r_.T[...], pd) + dot(r_.S[...], tab_e) + r_.ce[l])
        r_.gate[l] = gate
        num = select_rows(r_.TT[...], gate * bs)
        den = select_rows(r_.TT[...], gate)
        r_.num[l] = num
        r_.den[l] = den
        msg = pa + num / (den + GATE_EPS)
        r_.z0[l] = msg
        mean0 = col_sum(msg) / R
        sync_start(3 * l, mean0, col_sum((msg - mean0) * (msg - mean0)))

    def forward(l, carry):
        def ready(js):
            for j in js:
                moved = (r_.gb[l, j].astype(F32) + r_.moff[j, 0:1]) * r_.move[0:1] + r_.move[1:2]
                r_.xs[l, j] = moved.astype(BF16)

        r_.xs[l, me] = r_.xf[l].astype(BF16)
        prepare_queries(l)
        arrive(r_.gb.at[l, 2 * z_from(1) + par], r_.agc_r.at[l, 1])
        gather_take(l, 0)
        gather_take(l, 1)
        ready([partner, 2 * z_from(1) + par, 2 * z_from(1) + 1 - par])

        def middle(i, hf):
            when((i == 0) & (hf == 0), *[functools.partial(gather_pass, l, t) for t in range(2, NZ)])

        def block(i, carry):
            attention_block(l, i, middle)

            @pl.when(i == 0)
            def _():
                for t in range(2, NZ):
                    gather_take(l, t)
                ready([2 * z_from(t) + p for t in range(2, NZ) for p in range(2)])
                convolution(l)

            return carry

        lax.fori_loop(0, NB, block, 0)
        mean1, sq1 = attention_end(l)
        sync_start(3 * l + 1, mean1, sq1)
        mean0, sq0 = sync_moments(3 * l)
        inv0 = lax.rsqrt(sq0 / total + NORM_EPS)
        r_.iv[l, 0:1] = inv0
        z0 = (r_.z0[l] - mean0) * inv0
        r_.z0[l] = z0
        n0 = z0 * r_.gain[l, 0:1] + r_.shift[l, 0:1]
        r_.local[...] = r_.xf[l] + n0 * sigmoid(n0)
        mean1, sq1 = sync_moments(3 * l + 1)
        inv1 = lax.rsqrt(sq1 / total + NORM_EPS)
        r_.iv[l, 1:2] = inv1
        z1 = (r_.z1[l] - mean1) * inv1
        r_.z1[l] = z1
        mix = r_.local[...] + z1 * r_.gain[l, 1:2] + r_.shift[l, 1:2]
        mb = mix.astype(BF16)
        r_.mb[l] = mb
        u = dot(mb, r_.wu[l])
        r_.u[l] = u
        g = (u * sigmoid(u)).astype(BF16)
        r_.g[l] = g
        y = mix + dot(g, r_.wd[l])
        r_.z2[l] = y
        mean = col_sum(y) / R
        cent = y - mean
        k = 3 * l + 2
        sync_start(k, mean, col_sum(cent * cent))

        @pl.when(l < L - 1)
        def _():
            r_.gb[l + 1, me] = cent.astype(BF16)
            gather_start(l + 1)

        @pl.when(l == L - 1)
        def _():
            dy = r_.cot[...].astype(F32)
            sync_start(3 * L, col_sum(dy), col_sum(dy * cent))

        tot_mean, tot_sq = sync_moments(k)
        inv2 = lax.rsqrt(tot_sq / total + NORM_EPS)
        r_.iv[l, 2:3] = inv2
        z2 = (r_.z2[l] - tot_mean) * inv2
        r_.z2[l] = z2
        gain, shift = r_.gain[l, 2:3], r_.shift[l, 2:3]
        r_.xf[l + 1] = z2 * gain + shift

        @pl.when(l == L - 1)
        def _():
            sync_wait(3 * L)
            sums, means = r_.st1[3 * L], r_.st1[k][:, 0:2]
            mean = jnp.mean(means, 0)
            dy_sum = jnp.sum(sums[:, 0:2], 0)
            dy_cent = jnp.sum(sums[:, 2:4] + (means - mean) * sums[:, 0:2], 0)
            dy_sum, dy_cent = unpack(jnp.concatenate([dy_sum, dy_cent], 0))
            r_.gshift[l, 2:3] = dy_sum
            r_.ggain[l, 2:3] = dy_cent * inv2

        for j in range(N):
            tile = r_.st1[k, rep * N + j]
            r_.moff[j, 0:1] = jnp.concatenate([tile[0:1], tile[1:2]], 1) - tot_mean
        r_.move[0:1] = inv2 * gain
        r_.move[1:2] = shift
        return carry

    lax.fori_loop(0, L, forward, 0)
    act_copy = pltpu.make_async_copy(r_.xf.at[L], r_.out_act, r_.store.at[0])
    act_copy.start()

    def back_feed_forward(l, k):
        s2, g2 = r_.gshift[l, 2:3], r_.ggain[l, 2:3]
        d3 = r_.gain[l, 2:3] * r_.iv[l, 2:3] * (r_.dy[...] - s2 / total - r_.z2[l] * (g2 / total))
        db = d3.astype(BF16)
        dub = (dot_nt(db, r_.wd[l]) * silu_slope(r_.u[l])).astype(BF16)
        dmix = d3 + dot_nt(dub, r_.wu[l])
        r_.dmix[...] = dmix
        n0 = r_.z0[l] * r_.gain[l, 0:1] + r_.shift[l, 0:1]
        gy0 = dmix * silu_slope(n0)
        sync_start(k, col_sum(dmix), col_sum(dmix * r_.z1[l]))
        sync_start(k + 1, col_sum(gy0), col_sum(gy0 * r_.z0[l]))
        r_.gy0[...] = gy0
        at = put(r_.gs_early, l, 512, dot_tn(r_.mb[l], dub))
        put(r_.gs_early, l, at, dot_tn(r_.g[l], db))
        r_.vT[...] = r_.vv[l].T
        r_.xeT[...] = r_.xe[l].T
        for hf in range(2):
            r_.qmT[hf] = r_.qm[l, hf].T

    def back_norms(l, k):
        s1, g1 = sync_sums(k)
        r_.gshift[l, 1:2] = s1
        r_.ggain[l, 1:2] = g1
        dmix = r_.dmix[...]
        d2 = r_.gain[l, 1:2] * r_.iv[l, 1:2] * (dmix - s1 / total - r_.z1[l] * (g1 / total))
        dab = d2.astype(BF16)
        r_.dxo[...] = dmix + d2
        r_.dob[...] = dot_nt(dab, r_.wo[l]).astype(BF16).astype(F32)
        put(r_.gs_early, l, 0, dot_tn(r_.ob[l], dab))
        r_.gkv[...] = jnp.zeros((2 * D, D), F32)
        r_.dq[...] = jnp.zeros((R, D), F32)

    def back_attention_block(l, i, between):
        t1 = (i + 1) % NB
        half = (zh + t1) % NB
        rows = pl.ds(pl.multiple_of(half * W, 128), W)

        def heads(hf, carry):
            lanes = lane_half(hf)
            dos = r_.dob[:, lanes] * r_.rb[l, (NB - t1) % NB, :, lanes]
            prod = dos * r_.oraw[l, :, lanes]
            for k in range(HK):
                r_.dom[k * R : (k + 1) * R] = jnp.where(lane_head == k, dos, 0.0).astype(BF16)
            parts = []
            for c in range(HK // 2):
                both = slice(2 * c * R, 2 * (c + 1) * R)
                dp = dot(r_.dom[both], r_.vT[lanes, rows])
                for k in range(2):
                    h = 2 * c + k
                    delta = jnp.sum(jnp.where(lane_head == h, prod, 0.0), 1, keepdims=True)
                    ds = r_.pst[l, head_rows(hf, h), rows].astype(F32) * (dp[k * R : (k + 1) * R] - delta)
                    r_.dss[h * R : (h + 1) * R] = ds.astype(BF16)
                part = dot(r_.dss[both], r_.kk[l, rows, lanes])
                parts += [part[0:R], part[R : 2 * R]]
            r_.dq[:, lanes] += by_head(parts)
            dk = dot(r_.qmT[hf], r_.dss[...]) * scale
            r_.dkv[pl.ds(pl.multiple_of(hf * 128, 128), 128)] = dk.astype(BF16)
            dv = dot(r_.dom[...].T, r_.pst[l, head_rows(hf, 0, HK), rows])
            r_.dkv[pl.ds(pl.multiple_of(D + hf * 128, 128), 128)] = dv.astype(BF16)
            between(i, hf)
            return carry

        lax.fori_loop(0, 2, heads, 0)
        dx = dot(r_.wqkv[l, :, D:], r_.dkv[...]).T
        r_.dxs[l, pl.ds(2 * half, 2)] = dx.astype(BF16).reshape(2, 2, R, D)

        @pl.when(i < NB - 1)
        def _():
            for low in range(2):
                zb = 2 * half + low
                send_rows(r_.dxs.at[l, zb, 1 - par], r_.rs1.at[l, zb], R,
                     r_.rsp_s.at[l, 2 * i + low], r_.rsp_r.at[l, 2 * i + low], nodes=partner)

        @pl.when(i == NB - 1)
        def _():
            near = z_to(1)
            send_rows(r_.dxs.at[l, z, 1 - par], r_.ro.at[l, 0], R, r_.ro_s.at[l, 0], r_.ro_r.at[l, 0], nodes=partner)
            send_rows(r_.dxs.at[l, near, par], r_.ro.at[l, 1], R, r_.ro_s.at[l, 1], r_.ro_r.at[l, 1], nodes=2 * near + par)
            send_rows(r_.dxs.at[l, near, 1 - par], r_.ro.at[l, 2], R, r_.ro_s.at[l, 2], r_.ro_r.at[l, 2],
                 nodes=2 * near + 1 - par)

        r_.gkv[...] += dot(r_.dkv[...], r_.xs[l, pl.ds(4 * half, 4)].reshape(W, D))

    def pass_on(l, i, t):
        zb = z_to(t)
        arrive(r_.rs1.at[l, zb], r_.rsp_r.at[l, 2 * i + zb % 2])
        both = r_.dxs[l, zb, par].astype(F32) + r_.rs1[l, zb].astype(F32)
        r_.cs[l, zb] = both.astype(BF16)
        send_rows(r_.cs.at[l, zb], r_.rs2.at[l, z], R, r_.rsc_s.at[l, t], r_.rsc_r.at[l, t], nodes=2 * zb + par)

    def back_convolution(l, k):
        s0, g0 = sync_sums(k + 1)
        r_.gshift[l, 0:1] = s0
        r_.ggain[l, 0:1] = g0
        inv_den = 1.0 / (r_.den[l] + GATE_EPS)
        dm = r_.gain[l, 0:1] * r_.iv[l, 0:1] * (r_.gy0[...] - s0 / total - r_.z0[l] * (g0 / total))
        dnum = dm * inv_den
        dden = -dnum * r_.num[l] * inv_den
        dnum_e = select_rows(r_.T[...], dnum)
        dden_e = select_rows(r_.T[...], dden)
        gate = r_.gate[l]
        dgp = (dnum_e * r_.bs[l].astype(F32) + dden_e) * gate * (1.0 - gate)
        r_.dce[...] = dgp.astype(BF16)
        dpb = select_rows(r_.ST[...], dnum_e * gate).astype(BF16)
        dpe = select_rows(r_.ST[...], dgp).astype(BF16)
        dpd = select_rows(r_.TT[...], dgp).astype(BF16)
        dmb = dm.astype(BF16)
        dxe = dot_nt(dpb, r_.wp[l, :, D : 2 * D]) + dot_nt(dpe, r_.wp[l, :, 3 * D :])
        r_.hs[l, 0] = dxe[R : R + 32].astype(BF16)
        r_.hs[l, 1] = dxe[R + 32 : R + 64].astype(BF16)
        send(r_.hs.at[l, 0], r_.hr.at[l, 1], r_.hal_s.at[l, 0], r_.hal_r.at[l, 0], nodes=prev)
        send(r_.hs.at[l, 1], r_.hr.at[l, 0], r_.hal_s.at[l, 1], r_.hal_r.at[l, 1], nodes=nxt)
        r_.dxo[...] += (
            dxe[0:R]
            + dot_nt(dmb, r_.wp[l, :, 0:D])
            + dot_nt(dpd, r_.wp[l, :, 2 * D : 3 * D])
        )
        r_.dproj[0, 0:R] = dmb
        r_.dproj[1] = dpb
        r_.dproj[2, 0:R] = dpd
        r_.dproj[3] = dpe

    def conv_weight_grads(l):
        at = 0
        for c in range(4):
            width = R if c % 2 == 0 else 256
            at = put(r_.gs_conv, l, at, dot(r_.xeT[:, 0:width], r_.dproj[c, 0:width]))
        put(r_.gs_conv, l, at, dot(r_.efT[...], r_.dce[...]))

    def back_input(l):
        dx = r_.dxo[...]
        dx = dx + r_.dxs[l, z, par].astype(F32)
        for slot in range(3):
            arrive(r_.ro.at[l, slot], r_.ro_r.at[l, slot])
            dx = dx + r_.ro[l, slot].astype(F32)
        for t in range(2, NZ):
            c = z_from(t)
            arrive(r_.rs2.at[l, c], r_.rsc_r.at[l, t])
            dx = dx + r_.rs2[l, c].astype(F32)
        arrive(r_.hr.at[l, 0], r_.hal_r.at[l, 1])
        arrive(r_.hr.at[l, 1], r_.hal_r.at[l, 0])
        back = jnp.concatenate(
            [r_.hr[l, 0].astype(F32)[0:24], r_.hr[l, 1].astype(F32)[0:24], jnp.zeros((16, D), F32)], 0
        )
        return dx + dot(r_.A[...], back.astype(BF16))

    r_.dy[...] = r_.cot[...].astype(F32)

    E1, C1, Q1, E0, C0, Q0 = range(len(GROUPS))

    def steps(*pairs):
        return [functools.partial(reduce_step, g, k) for g, k in pairs]

    r_.dy[...] = r_.cot[...].astype(F32)

    def backward(b, carry):
        l = L - 1 - b
        first, last = b == 0, b == L - 1
        k = 3 * L + 1 + 2 * b
        conv = functools.partial(back_convolution, l, k)
        conv_grads = functools.partial(conv_weight_grads, l)
        back_feed_forward(l, k)
        back_norms(l, k)
        when(first, *steps((E1, 0)))
        when(last, *steps((E1, 3), (C1, 1), (Q1, 1), (E0, 0)), conv, conv_grads,
             *steps((C1, 2), (Q1, 2), (E1, 4), (E0, 1), (C0, 0)))

        def between(i, hf):
            when(first & (i == 0) & (hf == 0), *steps((E1, 1)))
            when(first & (i == 1) & (hf == 0), *steps((E1, 2)))
            when(last & (i == 0) & (hf == 0), *steps((C0, 1)))
            when(last & (i == 0) & (hf == 1), *steps((E0, 2), (C1, 3), (Q1, 3), (E1, 5)))
            when(last & (i == 1) & (hf == 0), *steps((E0, 3), (C0, 2), (C1, 4), (Q1, 4), (E1, 6)))
            when(last & (i == 1) & (hf == 1), *steps((E0, 4), (C1, 5), (Q1, 5)))
            for t in range(2, NZ):
                when((i == 1) & (hf == 0), functools.partial(pass_on, l, 0, t))

        def block(i, carry):
            back_attention_block(l, i, between)
            return carry

        lax.fori_loop(0, NB, block, 0)
        when(first, conv)
        dqb = (r_.dq[...] * scale).astype(BF16)
        r_.dxo[...] += dot_nt(dqb, r_.wqkv[l, :, 0:D])
        when(first, conv_grads, *steps((C1, 0)))
        at = put(r_.gs_qkv, l, 0, dot(r_.xeT[:, 0:R], dqb))
        put(r_.gs_qkv, l, at, r_.gkv[...].T)

        @pl.when(first)
        def _():
            dx = back_input(l)
            r_.dy[...] = dx
            below = L - 2
            sync_start(SYNCS - 1, col_sum(dx), col_sum(dx * r_.z2[below]))
            reduce_step(Q1, 0)
            s2, g2 = sync_sums(SYNCS - 1)
            r_.gshift[below, 2:3] = s2
            r_.ggain[below, 2:3] = g2

        return carry

    lax.fori_loop(0, L, backward, 0)
    for step in steps((Q0, 0), (C0, 3), (E0, 5), (C1, 6), (Q1, 6), (Q0, 1)):
        step()
    r_.dy[...] = back_input(0)
    in_copy = pltpu.make_async_copy(r_.dy, r_.grad_in, r_.store.at[1])
    in_copy.start()
    for step in steps(
        (C0, 4), (E0, 6), (C1, 7), (Q0, 2),
        (C0, 5), (E0, 7), (C1, 8), (Q0, 3),
        (C0, 6), (E0, 8), (Q0, 4),
    ):
        step()
    for l in range(L):
        for k in range(3):
            r_.ggain_out[k, l : l + 1] = r_.ggain[l, k : k + 1]
            r_.gshift_out[k, l : l + 1] = r_.gshift[l, k : k + 1]
    for g in range(len(GROUPS)):
        reduce_drain(g)
    sent(r_.meta.at[0 : N - 1], r_.meta_s.at[0])
    for k in range(SYNCS):
        sent(r_.st1.at[k, 0 : M * N - 1], r_.st1_s.at[k])
    for l in range(L):
        for t in range(NZ):
            sent(r_.gb.at[l, 0], r_.agp_s.at[l, t])
            if t > 0:
                sent(r_.gb.at[l, 0], r_.agc_s.at[l, t])
            if t > 1:
                sent(r_.rs1.at[l, 0], r_.rsc_s.at[l, t])
        for slot in range(2 * (NB - 1)):
            sent(r_.rs1.at[l, 0], r_.rsp_s.at[l, slot])
        for slot in range(3):
            sent(r_.ro.at[l, 0], r_.ro_s.at[l, slot])
        for side in range(2):
            sent(r_.hs.at[l, 0], r_.hal_s.at[l, side])
    act_copy.wait()
    in_copy.wait()


def finish_kernel(act_h, gin_h, *refs):
    n = len(GROUPS)
    held, (ggain_h, gshift_h), refs = refs[:n], refs[n : n + 2], refs[n + 2 :]
    act_o, gin_o, proj_o, edge_o, qkv_o, out_o, up_o, down_o, ggain_o, gshift_o = refs[:10]
    summed, refs = refs[10 : 10 + n], refs[10 + n :]
    act, gin, proj, edge, qkv, out, up, down, in_sem, out_sem = refs
    loads = [
        pltpu.make_async_copy(src, dst, in_sem.at[i])
        for i, (src, dst) in enumerate(zip(held + (act_h, gin_h), summed + (act, gin), strict=True))
    ]
    for load in loads:
        load.start()
    ggain_o[...] = ggain_h[...]
    gshift_o[...] = gshift_h[...]
    stores = []

    def store(src, dst):
        copy = pltpu.make_async_copy(src, dst, out_sem.at[len(stores)])
        copy.start()
        stores.append(copy)

    def widen(dst, l, g, at, first=0, last=None):
        rows = dst.shape[1]
        for c in range(first, dst.shape[2] // 128 if last is None else last):
            dst[l, :, 128 * c : 128 * (c + 1)] = summed[g][at : at + rows].astype(F32)
            at += rows
        return at

    for g, (name, l, first, rows, _) in enumerate(GROUPS):
        loads[g].wait()
        if name == "early":
            at = widen(out, l, g, 0)
            store(out.at[l], out_o.at[l])
            at = widen(up, l, g, at)
            store(up.at[l], up_o.at[l])
            widen(down, l, g, at)
            store(down.at[l], down_o.at[l])
        elif name == "conv":
            at = widen(proj, l, g, 0)
            store(proj.at[l], proj_o.at[l])
            widen(edge, l, g, at)
            store(edge.at[l], edge_o.at[l])
        else:
            widen(qkv, l, g, 0, first // 256, (first + rows) // 256)
            if first + rows == 1536:
                store(qkv.at[l], qkv_o.at[l])
    for i, (src, dst) in enumerate(((act, act_o), (gin, gin_o))):
        loads[n + i].wait()
        store(src, dst)
    for copy in stores:
        copy.wait()


def fused_device(
    N, M, node_input, edge_feat, graph_ids, edge_src, edge_dst, halo_send, w_proj, w_edge, w_qkv,
    w_out, w_up, w_down, norm_gain, norm_shift, cotangent,
):
    R, D = node_input.shape
    E = edge_feat.shape[0]
    L = w_proj.shape[0]
    names = scratch_list(N, M, L, R, E)
    vmem = pl.BlockSpec(memory_space=pltpu.VMEM)
    hbm = pl.BlockSpec(memory_space=pltpu.HBM)
    shape = jax.ShapeDtypeStruct
    rows = shape((R, D), F32)
    norm = shape((3, L, D), F32)
    groups = [shape((rows_g, 128), BF16) for _, _, _, rows_g, _ in GROUPS]
    outs = pl.pallas_call(
        functools.partial(kernel, N, M, L, tuple(names)),
        out_shape=[rows, rows, *groups, norm, norm],
        in_specs=[hbm] + [vmem] * 4 + [hbm] * 7 + [vmem] * 2 + [hbm],
        out_specs=[hbm] * (2 + len(GROUPS)) + [vmem] * 2,
        scratch_shapes=list(names.values()),
        compiler_params=pltpu.CompilerParams(
            collective_id=0, has_side_effects=True, vmem_limit_bytes=60 << 20
        ),
        name="layers",
    )(node_input, graph_ids, edge_src, edge_dst, halo_send, edge_feat, w_proj, w_edge, w_qkv, w_out, w_up,
      w_down, norm_gain.transpose(1, 0, 2), norm_shift.transpose(1, 0, 2), cotangent)
    weights = [shape(w.shape, F32) for w in (w_proj, w_edge, w_qkv, w_out, w_up, w_down)]
    results = pl.pallas_call(
        finish_kernel,
        out_shape=[rows, rows, *weights, norm, norm],
        in_specs=[hbm] * (2 + len(GROUPS)) + [vmem] * 2,
        out_specs=[hbm] * 8 + [vmem] * 2,
        scratch_shapes=[pltpu.VMEM(s.shape, s.dtype) for s in (*groups, rows, rows, *weights)]
        + [pltpu.SemaphoreType.DMA((len(GROUPS) + 2,)), pltpu.SemaphoreType.DMA((14,))],
        compiler_params=pltpu.CompilerParams(vmem_limit_bytes=60 << 20),
        name="gradients",
    )(*outs)
    ggain, gshift = results[8].transpose(1, 0, 2), results[9].transpose(1, 0, 2)
    return (*results[:8], ggain, gshift)


BLOCK_CAP = 2048


def extended_2(block, sides, width):
    for axis, dim in sides:
        count = lax.axis_size(axis)
        forward = [(i, i + 1) for i in range(count - 1)]
        forward.append((count - 1, 0))
        backward = [(target, source) for source, target in forward]
        low = lax.ppermute(
            lax.slice_in_dim(block, block.shape[dim] - width, None, axis=dim), axis, forward
        )
        high = lax.ppermute(lax.slice_in_dim(block, 0, width, axis=dim), axis, backward)
        block = jnp.concatenate([low, block, high], axis=dim)
    return block


def block_length(total_rows, upper_limit):
    for length in range(min(total_rows, upper_limit), 0, -1):
        if total_rows % length == 0:
            return length
    return 1


def outer_product(left, right):
    return lax.dot_general(
        left, right, (((0,), (0,)), ((), ())), preferred_element_type=jnp.float32
    )


def times_transposed(left, weight):
    return lax.dot_general(
        left, weight, (((1,), (1,)), ((), ())), preferred_element_type=jnp.float32
    )


def forward_product(left, weight):
    return jnp.dot(left, weight, preferred_element_type=jnp.float32)


def silu_slope_plain(inputs):
    logistic = jax.nn.sigmoid(inputs)
    return logistic * (1.0 + inputs * (1.0 - logistic))


def normalize(inputs, gain_row, shift_row, node_total):
    batch_mean = lax.psum(jnp.sum(inputs, 0), ("nodes", "rep")) / node_total
    centred = inputs - batch_mean
    batch_var = lax.psum(jnp.sum(centred * centred, 0), ("nodes", "rep")) / node_total
    inv_std = lax.rsqrt(batch_var + NORM_EPS)
    standard = (inputs - batch_mean) * inv_std
    return (standard * gain_row + shift_row, standard, inv_std)


def normalize_back(grad_out, standard, inv_std, gain_row, node_total):
    shift_grad, gain_grad = lax.psum(
        (jnp.sum(grad_out, 0), jnp.sum(grad_out * standard, 0)), ("nodes", "rep")
    )
    grad_in = (
        gain_row
        * inv_std
        * (grad_out - shift_grad / node_total - standard * gain_grad / node_total)
    )
    return (grad_in, gain_grad, shift_grad)


def exchange_sources(outgoing):
    halo_rows = outgoing.shape[0] // 2
    grown = extended_2(outgoing, (("nodes", 0),), halo_rows)
    return jnp.concatenate([grown[:halo_rows], grown[3 * halo_rows :]], 0)


def return_sources(incoming_grad):
    halo_rows = incoming_grad.shape[0] // 2
    grown = extended_2(incoming_grad.astype(jnp.bfloat16), (("nodes", 0),), halo_rows).astype(
        incoming_grad.dtype
    )
    return jnp.concatenate([grown[:halo_rows], grown[3 * halo_rows :]], 0)


def attend_forward(query_rows, key_rows, value_rows, local_graphs, group_graphs):
    row_count = query_rows.shape[0]
    score_scale = HEAD_DIM ** (-0.5)
    queries = query_rows.reshape(row_count, HEADS, HEAD_DIM)

    def add_piece(carried, kv_piece, first_row):
        key_piece, value_piece = kv_piece
        piece_rows = key_piece.shape[0]
        block_len = block_length(piece_rows, BLOCK_CAP)

        def add_block(block_state, block_index):
            row_max, row_sum, accumulated = block_state
            block_start = block_index * block_len
            key_block = lax.dynamic_slice_in_dim(key_piece, block_start, block_len, 0).reshape(
                block_len, HEADS, HEAD_DIM
            )
            value_block = lax.dynamic_slice_in_dim(value_piece, block_start, block_len, 0).reshape(
                block_len, HEADS, HEAD_DIM
            )
            key_graphs = lax.dynamic_slice_in_dim(
                group_graphs, first_row + block_start, block_len, 0
            )
            same_graph = (local_graphs[:, None] == key_graphs[None, :])[None]
            scores = (
                jnp.einsum("qhd,khd->hqk", queries, key_block, preferred_element_type=jnp.float32)
                * score_scale
            )
            scores = jnp.where(same_graph, scores, NEG)
            new_max = jnp.maximum(row_max, jnp.max(scores, 2))
            weights = jnp.where(same_graph, jnp.exp(scores - new_max[:, :, None]), 0.0)
            factor = jnp.exp(row_max - new_max)
            row_sum = row_sum * factor + jnp.sum(weights, 2)
            contrib = jnp.einsum(
                "hqk,khd->qhd",
                weights.astype(jnp.bfloat16),
                value_block,
                preferred_element_type=jnp.float32,
            )
            accumulated = accumulated * jnp.transpose(factor)[:, :, None] + contrib
            return ((new_max, row_sum, accumulated), None)

        carried, _ = lax.scan(add_block, carried, jnp.arange(piece_rows // block_len))
        return carried

    start_state = (
        jnp.full((HEADS, row_count), NEG, jnp.float32),
        jnp.zeros((HEADS, row_count), jnp.float32),
        jnp.zeros((row_count, HEADS, HEAD_DIM), jnp.float32),
    )
    row_max, row_sum, accumulated = add_piece(
        start_state,
        (
            lax.all_gather(key_rows, "nodes", axis=0, tiled=True),
            lax.all_gather(value_rows, "nodes", axis=0, tiled=True),
        ),
        jnp.int32(0),
    )
    attn_raw = accumulated / jnp.transpose(row_sum)[:, :, None]
    log_sum = row_max + jnp.log(row_sum)
    return (attn_raw, log_sum)


def attend_backward(
    query_rows, key_rows, value_rows, grad_low, attn_raw, log_sum, local_graphs, group_graphs
):
    row_count = query_rows.shape[0]
    model_width = HEADS * HEAD_DIM
    score_scale = HEAD_DIM ** (-0.5)
    queries = query_rows.reshape(row_count, HEADS, HEAD_DIM)
    grad_heads = grad_low.reshape(row_count, HEADS, HEAD_DIM)
    row_delta = jnp.einsum("qhd,qhd->hq", grad_heads.astype(jnp.float32), attn_raw)

    def score_block(key_block, value_block, key_graphs):
        same_graph = (local_graphs[:, None] == key_graphs[None, :])[None]
        scores = (
            jnp.einsum("qhd,khd->hqk", queries, key_block, preferred_element_type=jnp.float32)
            * score_scale
        )
        attn_weights = jnp.exp(jnp.where(same_graph, scores - log_sum[:, :, None], NEG))
        grad_weights = jnp.einsum(
            "qhd,khd->hqk", grad_heads, value_block, preferred_element_type=jnp.float32
        )
        grad_scores = (attn_weights * (grad_weights - row_delta[:, :, None])).astype(jnp.bfloat16)
        return (attn_weights, grad_scores)

    def key_terms(attn_weights, grad_scores, block_len):
        grad_keys = (
            jnp.einsum("hqk,qhd->khd", grad_scores, queries, preferred_element_type=jnp.float32)
            * score_scale
        )
        grad_values = jnp.einsum(
            "hqk,qhd->khd",
            attn_weights.astype(jnp.bfloat16),
            grad_heads,
            preferred_element_type=jnp.float32,
        )
        return jnp.concatenate(
            [
                grad_keys.reshape(block_len, model_width),
                grad_values.reshape(block_len, model_width),
            ],
            1,
        )

    def query_term(grad_scores, key_block):
        return (
            jnp.einsum("hqk,khd->qhd", grad_scores, key_block, preferred_element_type=jnp.float32)
            * score_scale
        )

    group_rows = group_graphs.shape[0]

    def add_piece(carried, kv_piece, first_row):
        key_piece, value_piece = kv_piece
        piece_rows = key_piece.shape[0]
        block_len = block_length(piece_rows, BLOCK_CAP)

        def add_block(block_state, block_index):
            grad_query, buffer = block_state
            block_start = block_index * block_len
            key_block = lax.dynamic_slice_in_dim(key_piece, block_start, block_len, 0).reshape(
                block_len, HEADS, HEAD_DIM
            )
            value_block = lax.dynamic_slice_in_dim(value_piece, block_start, block_len, 0).reshape(
                block_len, HEADS, HEAD_DIM
            )
            place = first_row + block_start
            key_graphs = lax.dynamic_slice_in_dim(group_graphs, place, block_len, 0)
            attn_weights, grad_scores = score_block(key_block, value_block, key_graphs)
            grad_query = grad_query + query_term(grad_scores, key_block)
            block_terms = key_terms(attn_weights, grad_scores, block_len)
            current = lax.dynamic_slice_in_dim(buffer, place, block_len, 0)
            buffer = lax.dynamic_update_slice_in_dim(buffer, current + block_terms, place, 0)
            return ((grad_query, buffer), None)

        carried, _ = lax.scan(add_block, carried, jnp.arange(piece_rows // block_len))
        return carried

    start_state = (
        jnp.zeros((row_count, HEADS, HEAD_DIM), jnp.float32),
        jnp.zeros((group_rows, 2 * model_width), jnp.float32),
    )
    grad_query, buffer = add_piece(
        start_state,
        (
            lax.all_gather(key_rows, "nodes", axis=0, tiled=True),
            lax.all_gather(value_rows, "nodes", axis=0, tiled=True),
        ),
        jnp.int32(0),
    )
    grad_kv = lax.psum_scatter(buffer, "nodes", scatter_dimension=0, tiled=True)
    return (
        grad_query.reshape(row_count, model_width),
        grad_kv[:, :model_width],
        grad_kv[:, model_width:],
    )


def layer_forward(
    hidden, params, edge_feat, edge_src, edge_dst, halo_send, local_graphs, group_graphs, node_total
):
    w_proj, w_edge, w_qkv, w_out, w_up, w_down, norm_gains, norm_shifts = params
    row_count, model_width = hidden.shape
    hidden_low = hidden.astype(jnp.bfloat16)
    projected = forward_product(hidden_low, w_proj)
    self_term = projected[:, :model_width]
    dest_term = projected[:, 2 * model_width : 3 * model_width]
    source_rows = jnp.concatenate(
        [projected[:, model_width : 2 * model_width], projected[:, 3 * model_width :]], 1
    ).astype(jnp.bfloat16)
    incoming = exchange_sources(source_rows[halo_send])
    extended = jnp.concatenate([source_rows, incoming], 0)
    edge_rows = extended[edge_src].astype(jnp.float32)
    source_b = edge_rows[:, :model_width]
    source_e = edge_rows[:, model_width:]
    edge_proj = forward_product(edge_feat, w_edge)
    gating = jax.nn.sigmoid(dest_term[edge_dst] + source_e + edge_proj)
    numerator = jax.ops.segment_sum(gating * source_b, edge_dst, row_count)
    denominator = jax.ops.segment_sum(gating, edge_dst, row_count)
    message = self_term + numerator / (denominator + GATE_EPS)
    normed_one, standard_one, inv_one = normalize(
        message, norm_gains[0], norm_shifts[0], node_total
    )
    local_out = hidden + jax.nn.silu(normed_one)
    qkv_low = forward_product(hidden_low, w_qkv).astype(jnp.bfloat16)
    query_rows = qkv_low[:, :model_width]
    key_rows = qkv_low[:, model_width : 2 * model_width]
    value_rows = qkv_low[:, 2 * model_width :]
    attn_raw, log_sum = attend_forward(query_rows, key_rows, value_rows, local_graphs, group_graphs)
    attn_low = attn_raw.reshape(row_count, model_width).astype(jnp.bfloat16)
    attn_proj = forward_product(attn_low, w_out)
    normed_two, standard_two, inv_two = normalize(
        hidden + attn_proj, norm_gains[1], norm_shifts[1], node_total
    )
    mixed = local_out + normed_two
    mixed_low = mixed.astype(jnp.bfloat16)
    up_proj = forward_product(mixed_low, w_up)
    activated = jax.nn.silu(up_proj).astype(jnp.bfloat16)
    down_proj = forward_product(activated, w_down)
    normed_three, standard_three, inv_three = normalize(
        mixed + down_proj, norm_gains[2], norm_shifts[2], node_total
    )
    saved = (
        hidden_low,
        source_b,
        gating,
        numerator,
        denominator,
        normed_one,
        standard_one,
        inv_one,
        query_rows,
        key_rows,
        value_rows,
        attn_raw,
        log_sum,
        attn_low,
        standard_two,
        inv_two,
        mixed_low,
        up_proj,
        activated,
        standard_three,
        inv_three,
    )
    return (normed_three, saved)


def layer_backward(
    grad_out,
    params,
    saved,
    edge_feat,
    edge_src,
    edge_dst,
    halo_send,
    local_graphs,
    group_graphs,
    node_total,
):
    w_proj, w_edge, w_qkv, w_out, w_up, w_down, norm_gains, norm_shifts = params
    (
        hidden_low,
        source_b,
        gating,
        numerator,
        denominator,
        normed_one,
        standard_one,
        inv_one,
        query_rows,
        key_rows,
        value_rows,
        attn_raw,
        log_sum,
        attn_low,
        standard_two,
        inv_two,
        mixed_low,
        up_proj,
        activated,
        standard_three,
        inv_three,
    ) = saved
    row_count, model_width = grad_out.shape
    grad_three, gain_three, shift_three = normalize_back(
        grad_out, standard_three, inv_three, norm_gains[2], node_total
    )
    down_grad = grad_three.astype(jnp.bfloat16)
    grad_w_down = outer_product(activated, down_grad)
    up_grad = (times_transposed(down_grad, w_down) * silu_slope_plain(up_proj)).astype(jnp.bfloat16)
    grad_w_up = outer_product(mixed_low, up_grad)
    grad_mixed = grad_three + times_transposed(up_grad, w_up)
    grad_two, gain_two, shift_two = normalize_back(
        grad_mixed, standard_two, inv_two, norm_gains[1], node_total
    )
    out_grad = grad_two.astype(jnp.bfloat16)
    grad_w_out = outer_product(attn_low, out_grad)
    attn_grad = times_transposed(out_grad, w_out).astype(jnp.bfloat16)
    grad_query, grad_key, grad_value = attend_backward(
        query_rows, key_rows, value_rows, attn_grad, attn_raw, log_sum, local_graphs, group_graphs
    )
    qkv_grad = jnp.concatenate([grad_query, grad_key, grad_value], 1).astype(jnp.bfloat16)
    grad_w_qkv = outer_product(hidden_low, qkv_grad)
    grad_message, gain_one, shift_one = normalize_back(
        grad_mixed * silu_slope_plain(normed_one), standard_one, inv_one, norm_gains[0], node_total
    )
    shifted = denominator + GATE_EPS
    grad_numer = grad_message / shifted
    grad_denom = -grad_message * numerator / (shifted * shifted)
    numer_edge = grad_numer[edge_dst]
    grad_gate = numer_edge * source_b + grad_denom[edge_dst]
    grad_pre_edge = grad_gate * gating * (1.0 - gating)
    edge_grad = grad_pre_edge.astype(jnp.bfloat16)
    grad_w_edge = outer_product(edge_feat, edge_grad)
    grad_dest = jax.ops.segment_sum(grad_pre_edge, edge_dst, row_count)
    grad_extended = jax.ops.segment_sum(
        jnp.concatenate([numer_edge * gating, grad_pre_edge], 1),
        edge_src,
        row_count + halo_send.shape[0],
    )
    returned = return_sources(grad_extended[row_count:])
    grad_source = grad_extended[:row_count].at[halo_send].add(returned)
    proj_grad = jnp.concatenate(
        [grad_message, grad_source[:, :model_width], grad_dest, grad_source[:, model_width:]], 1
    ).astype(jnp.bfloat16)
    grad_w_proj = outer_product(hidden_low, proj_grad)
    grad_hidden = (
        grad_mixed
        + grad_two
        + times_transposed(proj_grad, w_proj)
        + times_transposed(qkv_grad, w_qkv)
    )
    weight_grads = (grad_w_proj, grad_w_edge, grad_w_qkv, grad_w_out, grad_w_up, grad_w_down)
    return (
        grad_hidden,
        weight_grads,
        jnp.stack([gain_one, gain_two, gain_three]),
        jnp.stack([shift_one, shift_two, shift_three]),
    )


def per_device(
    node_input,
    edge_feat,
    graph_ids,
    edge_src,
    edge_dst,
    halo_send,
    w_proj,
    w_edge,
    w_qkv,
    w_out,
    w_up,
    w_down,
    norm_gain,
    norm_shift,
    cotangent,
):
    group_graphs = lax.all_gather(graph_ids, "nodes", axis=0, tiled=True)
    node_total = node_input.shape[0] * lax.axis_size("nodes") * lax.axis_size("rep")
    layer_count = w_proj.shape[0]
    layer_params = [
        (
            w_proj[layer_index],
            w_edge[layer_index],
            w_qkv[layer_index],
            w_out[layer_index],
            w_up[layer_index],
            w_down[layer_index],
            norm_gain[layer_index],
            norm_shift[layer_index],
        )
        for layer_index in range(layer_count)
    ]
    hidden = node_input.astype(jnp.float32)
    saved_all = []
    for layer_index in range(layer_count):
        hidden, saved = layer_forward(
            hidden,
            layer_params[layer_index],
            edge_feat,
            edge_src,
            edge_dst,
            halo_send,
            graph_ids,
            group_graphs,
            node_total,
        )
        saved_all.append(saved)
    grad_hidden = cotangent.astype(jnp.float32)
    weight_parts = [None] * layer_count
    gain_parts = [None] * layer_count
    shift_parts = [None] * layer_count
    for layer_index in range(layer_count - 1, -1, -1):
        (
            grad_hidden,
            weight_parts[layer_index],
            gain_parts[layer_index],
            shift_parts[layer_index],
        ) = layer_backward(
            grad_hidden,
            layer_params[layer_index],
            saved_all[layer_index],
            edge_feat,
            edge_src,
            edge_dst,
            halo_send,
            graph_ids,
            group_graphs,
            node_total,
        )
    proj_local = jnp.stack([weight_parts[layer_index][0] for layer_index in range(layer_count)])
    edge_local = jnp.stack([weight_parts[layer_index][1] for layer_index in range(layer_count)])
    qkv_local = jnp.stack([weight_parts[layer_index][2] for layer_index in range(layer_count)])
    out_local = jnp.stack([weight_parts[layer_index][3] for layer_index in range(layer_count)])
    up_local = jnp.stack([weight_parts[layer_index][4] for layer_index in range(layer_count)])
    down_local = jnp.stack([weight_parts[layer_index][5] for layer_index in range(layer_count)])
    grad_proj, grad_edge, grad_qkv, grad_out, grad_up, grad_down = lax.psum(
        (proj_local, edge_local, qkv_local, out_local, up_local, down_local), ("nodes", "rep")
    )
    return (
        hidden,
        grad_hidden,
        grad_proj,
        grad_edge,
        grad_qkv,
        grad_out,
        grad_up,
        grad_down,
        jnp.stack(gain_parts),
        jnp.stack(shift_parts),
    )


def solution(mesh):
    in_specs = (
        P(("rep", "nodes"), None),
        P(("rep", "nodes"), None),
        P(("rep", "nodes")),
        P(("rep", "nodes")),
        P(("rep", "nodes")),
        P(("rep", "nodes")),
        P(),
        P(),
        P(),
        P(),
        P(),
        P(),
        P(),
        P(),
        P(("rep", "nodes"), None),
    )
    out_specs = (
        P(("rep", "nodes"), None),
        P(("rep", "nodes"), None),
        P(),
        P(),
        P(),
        P(),
        P(),
        P(),
        P(),
        P(),
    )
    N, M = mesh.shape["nodes"], mesh.shape["rep"]
    fused = N in (4, 8) and M % 2 == 0 and 512 % (16 * N * M) == 0
    return jax.shard_map(
        functools.partial(fused_device, N, M) if fused else per_device,
        mesh=mesh, in_specs=in_specs, out_specs=out_specs, check_vma=False,
    )
```

```python
import functools
import math

import jax
import jax.numpy as jnp
from jax import lax
from jax.experimental import pallas as pl
from jax.experimental.pallas import tpu as pltpu
from jax.sharding import PartitionSpec as P

HEADS = 8
HEAD_DIM = 32
NEG = -1e30
NORM_EPS = 1e-05
GATE_EPS = 1e-06
F32, BF16, I32 = jnp.float32, jnp.bfloat16, jnp.int32
MESH = pl.DeviceIdType.MESH
SYNCS = 12
STRIP = 32
GROUPS = (
    ("early", 1, 0, 2560, ("core", "y", "nodes")),
    ("conv", 1, 0, 2560, ("core", "x", "y", "z")),
    ("qkv", 1, 0, 1536, ("core", "y", "nodes")),
    ("early", 0, 0, 2560, ("core", "x", "y", "z")),
    ("conv", 0, 0, 2560, ("core", "y", "nodes")),
    ("qkv", 0, 0, 1536, ("rep", "nodes")),
)


def dot(left, right):
    return lax.dot_general(
        left, right, (((1,), (0,)), ((), ())), preferred_element_type=F32
    )


def dot_nt(left, right):
    return lax.dot_general(
        left, right, (((1,), (1,)), ((), ())), preferred_element_type=F32
    )


def dot_tn(left, right):
    return lax.dot_general(
        left, right, (((0,), (0,)), ((), ())), preferred_element_type=F32
    )


def split(value):
    high = value.astype(BF16)
    return high, (value - high.astype(F32)).astype(BF16)


def sigmoid(value):
    return jax.nn.sigmoid(value)


def silu_slope(value):
    logistic = sigmoid(value)
    return logistic * (1.0 + value * (1.0 - logistic))


def col_sum(value):
    return jnp.sum(value, axis=0, keepdims=True)


def pack(first, second):
    return jnp.concatenate([first[:, :128], first[:, 128:], second[:, :128], second[:, 128:]], 0)


def unpack(tile):
    return [jnp.concatenate([tile[i : i + 1], tile[i + 1 : i + 2]], 1) for i in (0, 2)]


def combine_moments(tiles, count):
    mean = jnp.mean(tiles[:, 0:2], 0)
    off = tiles[:, 0:2] - mean
    return jnp.concatenate([mean, jnp.sum(tiles[:, 2:4] + count * off * off, 0)], 0)


class Refs:
    pass


def axis_sizes(N, M):
    return dict(core=2, y=M // 2, x=2, z=N // 2, rep=M, nodes=N)


def scratch_list(N, M, L, R, E):
    NZ, NB, G = N // 2, N // 4, N * R
    D, FF, W, HH = 256, 512, 4 * R, HEADS // 2 * R
    dma = lambda *shape: pltpu.SemaphoreType.DMA(shape)
    vm = lambda dtype, *shape: pltpu.VMEM(shape, dtype)
    names = dict(
        gb=vm(BF16, L, N, R, D),
        xs=vm(BF16, L, N, R, D),
        meta=vm(I32, N, 8, 256),
        cot=vm(BF16, R, D),
        wp=vm(BF16, L, D, 4 * D),
        we=vm(BF16, L, D, D),
        wqkv=vm(BF16, L, D, 3 * D),
        wo=vm(BF16, L, D, D),
        wu=vm(BF16, L, D, FF),
        wd=vm(BF16, L, FF, D),
        st1=vm(F32, SYNCS, M * N, 4, 128),
        gain=vm(F32, L, 8, D),
        shift=vm(F32, L, 8, D),
        ggain=vm(F32, L, 8, D),
        gshift=vm(F32, L, 8, D),
        iv=vm(F32, L, 8, D),
        moff=vm(F32, N, 8, D),
        move=vm(F32, 8, D),
        le=vm(BF16, E, 1024),
        re=vm(BF16, 1024, D),
        TT=vm(BF16, R, 2 * E),
        ST=vm(BF16, 256, E),
        efT=vm(BF16, D, E),
        HP=vm(BF16, 32, R),
        HN=vm(BF16, 32, R),
        A=vm(BF16, R, 64),
        bias=vm(F32, R, G),
        xf=vm(F32, L + 1, R, D),
        xe=vm(BF16, L, 256, D),
        xeT=vm(BF16, D, 256),
        gate=vm(F32, L, E, D),
        bs=vm(BF16, L, E, D),
        num=vm(F32, L, R, D),
        den=vm(F32, L, R, D),
        z0=vm(F32, L, R, D),
        z1=vm(F32, L, R, D),
        z2=vm(F32, L, R, D),
        kk=vm(BF16, L, G, D),
        vv=vm(BF16, L, G, D),
        kT=vm(BF16, D, G),
        vT=vm(BF16, D, G),
        od=vm(F32, NB, R, D),
        md=vm(F32, NB, R, D),
        ld=vm(F32, NB, R, D),
        rb=vm(F32, L, NB, R, D),
        pst=vm(BF16, L, HEADS * R, G),
        oraw=vm(F32, L, R, D),
        ob=vm(BF16, L, R, D),
        mb=vm(BF16, L, R, D),
        u=vm(F32, L, R, FF),
        g=vm(BF16, L, R, FF),
        dy=vm(F32, R, D),
        dmix=vm(F32, R, D),
        gy0=vm(F32, R, D),
        local=vm(F32, R, D),
        dxo=vm(F32, R, D),
        dob=vm(F32, R, D),
        dq=vm(F32, R, D),
        qm=vm(BF16, L, 2, HH, 128),
        qmT=vm(BF16, 2, 128, HH),
        dom=vm(BF16, HH, 256),
        sc=vm(F32, 2, max(2 * R, E), W),
        tp=vm(F32, HEADS // 2, R, 128),
        dss=vm(BF16, HH, W),
        dkv=vm(BF16, 2 * D, W),
        gkv=vm(F32, 2 * D, D),
        gg=vm(BF16, 2 * E, 2 * D),
        dn=vm(BF16, 512, 2 * D),
        dproj=vm(BF16, 256, 4 * D),
        dxs=vm(BF16, L, NZ, 2, R, D),
        rs1=vm(BF16, L, NZ, R, D),
        cs=vm(BF16, L, NZ, R, D),
        rs2=vm(BF16, L, NZ, R, D),
        ro=vm(BF16, L, 3, R, D),
        hs=vm(BF16, L, 2, 32, D),
        hr=vm(BF16, L, 2, 32, D),
    )
    names.update(
        gs_early=vm(BF16, L, 2560, 128),
        gs_conv=vm(BF16, L, 2560, 128),
        gs_qkv=vm(BF16, L, 1536, 128),
    )
    sizes = axis_sizes(N, M)
    for g, (_, _, _, rows, stages) in enumerate(GROUPS):
        names[f"go{g}"] = vm(BF16, rows, 128)
        left = rows
        for k, axis in enumerate(stages):
            left //= sizes[axis]
            names[f"ga{g}_{k}"] = vm(BF16, sizes[axis] - 1, left, 128)
            if k < len(stages) - 1:
                names[f"gh{g}_{k}"] = vm(BF16, left, 128)
    names.update(
        ar_s=dma(len(GROUPS), 8),
        ar_r=dma(len(GROUPS), 8),
        ar_l=dma(len(GROUPS)),
        load=dma(10),
        store=dma(2),
        meta_s=dma(1),
        meta_r=dma(1),
        st1_s=dma(SYNCS),
        st1_r=dma(SYNCS),
        agc_s=dma(L, NZ),
        agc_r=dma(L, NZ),
        agp_s=dma(L, NZ),
        agp_r=dma(L, NZ),
        rsp_s=dma(L, NZ),
        rsp_r=dma(L, NZ),
        ro_s=dma(L, 3),
        ro_r=dma(L, 3),
        rsc_s=dma(L, NZ),
        rsc_r=dma(L, NZ),
        hal_s=dma(L, 2),
        hal_r=dma(L, 2),
    )
    return names


IN_NAMES = (
    "x_in", "ids", "edge_src", "edge_dst", "halo", "ef_h", "wp_h", "we_h", "wqkv_h", "wo_h", "wu_h", "wd_h",
    "gain_in", "shift_in", "cot_h",
)
OUT_NAMES = ("out_act", "grad_in", *(f"gout{g}" for g in range(len(GROUPS))), "ggain_out", "gshift_out")


def kernel(N, M, L, names, *args):
    r_ = Refs()
    for name, ref in zip(IN_NAMES + OUT_NAMES + tuple(names), args, strict=True):
        setattr(r_, name, ref)
    R, D = r_.x_in.shape
    E = r_.ef_h.shape[0]
    NZ, NB, G, W = N // 2, N // 4, N * R, 4 * R
    HK = HEADS // 2
    total = float(N * M * R)
    scale = HEAD_DIM ** -0.5
    me = lax.axis_index("nodes")
    rep = lax.axis_index("rep")
    z = me // 2
    par = me % 2
    partner = 2 * z + (1 - par)
    prev = (me + N - 1) % N
    nxt = (me + 1) % N
    zh, zl = z // 2, z % 2
    z_to = lambda t: 2 * ((zh + t // 2) % NB) + (zl + t % 2) % 2
    z_from = lambda t: 2 * ((zh + NB - t // 2) % NB) + (zl + t % 2) % 2

    def remote(src, dst, s_sem, r_sem, **where):
        return pltpu.make_async_remote_copy(
            src_ref=src, dst_ref=dst, send_sem=s_sem, recv_sem=r_sem,
            device_id=where, device_id_type=MESH,
        )

    def send(src, dst, s_sem, r_sem, **where):
        remote(src, dst, s_sem, r_sem, **where).start()

    def send_rows(src, dst, rows, s_sem, r_sem, **where):
        pieces = next(p for p in range(1, rows) if rows % (16 * p) == 0 and rows // p <= 128)
        for at in range(0, rows, rows // pieces):
            cut = pl.ds(at, rows // pieces)
            send(src.at[cut], dst.at[cut], s_sem, r_sem, **where)

    def arrive(dst, r_sem):
        remote(dst, dst, r_sem, r_sem, nodes=partner).wait_recv()

    def sent(src, s_sem):
        remote(src, src, s_sem, s_sem, nodes=partner).wait_send()

    def when(condition, *acts):
        @pl.when(condition)
        def _():
            for act in acts:
                act()

    loads = [pltpu.make_async_copy(r_.ef_h, r_.le.at[:, D : 2 * D], r_.load.at[0])] + [
        pltpu.make_async_copy(getattr(r_, f"{name}_h"), getattr(r_, name), r_.load.at[1 + i])
        for i, name in enumerate(("we", "wqkv", "wp", "wo", "wu", "wd", "cot"))
    ]
    own_rows = pltpu.make_async_copy(r_.x_in, r_.gb.at[0, me], r_.load.at[8])
    own_rows.start()
    for load in loads:
        load.start()

    barrier = pltpu.get_barrier_semaphore()
    for dr in range(M):
        for d in range(N):
            if dr + d > 0:
                pl.semaphore_signal(barrier, inc=1, device_id={"rep": (rep + dr) % M, "nodes": (me + d) % N},
                                    device_id_type=MESH)
    pl.semaphore_wait(barrier, M * N - 1)

    def gather_start(l):
        mine = r_.gb.at[l, me]
        send_rows(mine, mine, R, r_.agp_s.at[l, 0], r_.agp_r.at[l, 0], nodes=partner)
        send_rows(mine, mine, R, r_.agc_s.at[l, 1], r_.agc_r.at[l, 1], nodes=2 * z_to(1) + par)
        send_rows(mine, mine, R, r_.agp_s.at[l, 1], r_.agp_r.at[l, 1], nodes=2 * z_to(1) + 1 - par)
        for t in range(2, NZ):
            send_rows(mine, mine, R, r_.agc_s.at[l, t], r_.agc_r.at[l, t], nodes=2 * z_to(t) + par)

    def gather_pass(l, t):
        piece = r_.gb.at[l, 2 * z_from(t) + par]
        arrive(piece, r_.agc_r.at[l, t])
        send_rows(piece, piece, R, r_.agp_s.at[l, t], r_.agp_r.at[l, t], nodes=partner)

    def gather_take(l, t):
        arrive(r_.gb.at[l, 2 * z_from(t) + 1 - par], r_.agp_r.at[l, t])

    def sync_start(k, first, second):
        mine = rep * N + me
        r_.st1[k, mine] = pack(first, second)
        for dr in range(M):
            for d in range(N):
                if dr + d > 0:
                    send(r_.st1.at[k, mine], r_.st1.at[k, mine], r_.st1_s.at[k], r_.st1_r.at[k],
                         rep=(rep + dr) % M, nodes=(me + d) % N)

    def sync_wait(k):
        arrive(r_.st1.at[k, 0 : M * N - 1], r_.st1_r.at[k])

    def sync_moments(k):
        sync_wait(k)
        return unpack(combine_moments(r_.st1[k], float(R)))

    def sync_sums(k):
        sync_wait(k)
        return unpack(jnp.sum(r_.st1[k], 0))

    sizes = axis_sizes(N, M)
    core, row = rep % 2, rep // 2
    places = dict(
        core=(core, lambda t: dict(rep=2 * row + t)),
        y=(row, lambda t: dict(rep=2 * t + core)),
        x=(par, lambda t: dict(nodes=2 * z + t)),
        z=(z, lambda t: dict(nodes=2 * t + par)),
        rep=(rep, lambda t: dict(rep=t)),
        nodes=(me, lambda t: dict(nodes=t)),
    )

    def reduce_step(g, step):
        name, layer, first, rows, stages = GROUPS[g]
        K = len(stages)
        gs, out = getattr(r_, f"gs_{name}").at[layer, first : first + rows], getattr(r_, f"go{g}")
        count, offset = [rows], [0]
        for axis in stages:
            count.append(count[-1] // sizes[axis])
            offset.append(offset[-1] + places[axis][0] * count[-1])
        take = lambda start, size: pl.ds(pl.multiple_of(start, 16), size)
        if 1 <= step <= K:
            k = step - 1
            got = getattr(r_, f"ga{g}_{k}")
            arrive(got, r_.ar_r.at[g, k])
            held = gs if k == 0 else getattr(r_, f"gh{g}_{k - 1}")
            index = places[stages[k]][0]
            acc = held[take(index * count[k + 1], count[k + 1])].astype(F32)
            for slot in range(sizes[stages[k]] - 1):
                acc = acc + got[slot].astype(F32)
            if step < K:
                getattr(r_, f"gh{g}_{k}")[...] = acc.astype(BF16)
            else:
                out[take(offset[K], count[K])] = acc.astype(BF16)
        elif step > K:
            k = 2 * K - step
            arrive(out.at[0 : (sizes[stages[k]] - 1) * count[k + 1]], r_.ar_r.at[g, step - 1])
        if step < K:
            held = gs if step == 0 else getattr(r_, f"gh{g}_{step - 1}")
            index, device = places[stages[step]]
            size = sizes[stages[step]]
            for d in range(1, size):
                to = (index + d) % size
                send_rows(held.at[take(to * count[step + 1], count[step + 1])], getattr(r_, f"ga{g}_{step}").at[d - 1],
                     count[step + 1], r_.ar_s.at[g, step], r_.ar_r.at[g, step], **device(to))
        elif step < 2 * K:
            k = 2 * K - 1 - step
            index, device = places[stages[k]]
            size = sizes[stages[k]]
            here = out.at[take(offset[k + 1], count[k + 1])]
            for d in range(1, size):
                send_rows(here, here, count[k + 1], r_.ar_s.at[g, step], r_.ar_r.at[g, step],
                          **device((index + d) % size))
        else:
            pltpu.make_async_copy(out, getattr(r_, f"gout{g}"), r_.ar_l.at[g]).start()

    def reduce_drain(g):
        _, _, _, rows, stages = GROUPS[g]
        K, left = len(stages), rows
        out = getattr(r_, f"go{g}")
        for k, axis in enumerate(stages):
            left //= sizes[axis]
            for step in (k, 2 * K - 1 - k):
                sent(out.at[0 : (sizes[axis] - 1) * left], r_.ar_s.at[g, step])
        pltpu.make_async_copy(out, getattr(r_, f"gout{g}"), r_.ar_l.at[g]).wait()

    def put(buf, l, at, value):
        rows = value.shape[0]
        for c in range(value.shape[1] // 128):
            buf[l, at : at + rows] = value[:, 128 * c : 128 * (c + 1)].astype(BF16)
            at += rows
        return at

    lane_head = lax.broadcasted_iota(I32, (R, 128), 1) // HEAD_DIM

    def by_head(parts):
        out = parts[0]
        for k in range(1, HK):
            out = jnp.where(lane_head == k, parts[k], out)
        return out

    r_.meta[me] = jnp.full((8, 256), -1, I32)
    r_.meta[me, 0:1, 0:R] = r_.ids[...].reshape(1, R)
    r_.meta[me, 1:2, 0:48] = r_.halo[...].reshape(1, 48)
    for d in range(1, N):
        send(r_.meta.at[me], r_.meta.at[me], r_.meta_s.at[0], r_.meta_r.at[0], nodes=(me + d) % N)
    own_rows.wait()
    gather_start(0)

    src_row = r_.edge_src[...].reshape(1, E)
    src_row = jnp.where(src_row < R + 24, src_row, src_row + 8)
    dst_row = r_.edge_dst[...].reshape(1, E)
    src_col = jnp.broadcast_to(src_row, (128, E)).T[:, 0:1]
    dst_col = jnp.broadcast_to(dst_row, (128, E)).T[:, 0:1]
    as_mask = lambda cond: cond.astype(F32).astype(BF16)
    r_.le[:, 0:256] = as_mask(src_col == lax.broadcasted_iota(I32, (E, 256), 1))
    target = as_mask(dst_col == lax.broadcasted_iota(I32, (E, 256), 1))
    r_.le[:, 512:768] = target
    r_.le[:, 768:1024] = target
    target = as_mask(dst_row == lax.broadcasted_iota(I32, (R, E), 0))
    r_.TT[:, 0:E] = target
    r_.TT[:, E:] = target
    r_.ST[...] = as_mask(src_row == lax.broadcasted_iota(I32, (256, E), 0))
    r_.dn[R:256] = jnp.zeros((256 - R, 2 * D), BF16)
    r_.dn[256 + R : 512] = jnp.zeros((256 - R, 2 * D), BF16)
    r_.dproj[R:256, 0:D] = jnp.zeros((256 - R, D), BF16)
    r_.dproj[R:256, 2 * D : 3 * D] = jnp.zeros((256 - R, D), BF16)
    loads[0].wait()
    r_.efT[...] = r_.le[:, D : 2 * D].T
    for l in range(L):
        for k in range(3):
            r_.gain[l, k : k + 1] = r_.gain_in[k, l : l + 1]
            r_.shift[l, k : k + 1] = r_.shift_in[k, l : l + 1]
    r_.xf[0] = r_.gb[0, me].astype(F32)
    r_.moff[...] = jnp.zeros((N, 8, D), F32)
    r_.move[0:1] = jnp.ones((1, D), F32)
    r_.move[1:2] = jnp.zeros((1, D), F32)
    for load in loads[1:]:
        load.wait()

    arrive(r_.meta.at[0 : N - 1], r_.meta_r.at[0])
    id_col = jnp.broadcast_to(r_.meta[me][0:1, 0:R], (128, R)).T[:, 0:1]
    id_row = jnp.concatenate([r_.meta[j][0:1, 0:R] for j in range(N)], 1)
    r_.bias[...] = jnp.where(id_col == id_row, 0.0, NEG)

    def halo_onehot(device, start):
        col = jnp.broadcast_to(r_.meta[device][1:2, 0:128], (128, 128)).T[start : start + 24, 0:1]
        hot = (col == lax.broadcasted_iota(I32, (24, R), 1)).astype(F32)
        return jnp.concatenate([hot, jnp.zeros((8, R), F32)], 0).astype(BF16)

    r_.HP[...] = halo_onehot(prev, 24)
    r_.HN[...] = halo_onehot(nxt, 0)
    r_.A[...] = as_mask(r_.meta[me][1:2, 0:64] == lax.broadcasted_iota(I32, (R, 64), 0))

    factor_exp = scale * math.log2(math.e)

    def prepare_queries(l):
        q = dot(r_.xs[l, me], r_.wqkv[l, :, :D]).astype(BF16).astype(F32)
        for hf in range(2):
            for k in range(HK):
                part = jnp.where(lane_head == k, q[:, 128 * hf : 128 * (hf + 1)], 0.0)
                r_.qm[l, hf, k * R : (k + 1) * R] = part.astype(BF16)

    def head_rows(hf, k, count=1):
        return pl.ds(pl.multiple_of((hf * HK + k) * R, 64), count * R)

    def lane_half(hf):
        return pl.ds(pl.multiple_of(hf * 128, 128), 128)

    def attention_block(l, i, middle):
        half = (zh + NB - i) % NB
        rows = pl.ds(pl.multiple_of(half * W, 128), W)
        x = r_.xs[l, pl.ds(4 * half, 4)].reshape(W, D)
        key = dot(x, r_.wqkv[l, :, D : 2 * D]).astype(BF16)
        r_.kk[l, rows] = key
        r_.kT[:, rows] = key.T
        r_.vv[l, rows] = dot(x, r_.wqkv[l, :, 2 * D :]).astype(BF16)

        def heads(hf, carry):
            lanes = lane_half(hf)
            sums, outs = [], []
            ones = jnp.ones((W, 128), BF16)
            for c in range(HK // 2):
                r_.sc[c % 2, 0 : 2 * R] = dot(r_.qm[l, hf, 2 * c * R : 2 * (c + 1) * R], r_.kT[lanes, rows])
                for k in range(2):
                    for at in range(0, R, STRIP):
                        s = r_.sc[c % 2, k * R + at : k * R + at + STRIP] + r_.bias[at : at + STRIP, rows]
                        top = jnp.max(s, 1, keepdims=True)
                        e = jnp.exp2((s - top) * factor_exp)
                        r_.tp[2 * c + k, at : at + STRIP] = jnp.broadcast_to(top, (STRIP, 128))
                        first = pl.multiple_of((hf * HK + 2 * c + k) * R + at, STRIP)
                        r_.pst[l, pl.ds(first, STRIP), rows] = e.astype(BF16)
                o = dot(r_.pst[l, head_rows(hf, 2 * c, 2), rows], jnp.concatenate([r_.vv[l, rows, lanes], ones], 1))
                for k in range(2):
                    outs.append(o[k * R : (k + 1) * R, 0:128])
                    sums.append(o[k * R : (k + 1) * R, 128:256])
            r_.md[i, :, lanes] = by_head([r_.tp[k] for k in range(HK)])
            r_.ld[i, :, lanes] = by_head(sums)
            r_.od[i, :, lanes] = by_head(outs)
            middle(i, hf)
            return carry

        lax.fori_loop(0, 2, heads, 0)

    def attention_end(l):
        top = r_.md[0]
        for i in range(1, NB):
            top = jnp.maximum(top, r_.md[i])
        factors = [jnp.exp2((r_.md[i] - top) * factor_exp) for i in range(NB)]
        inv = 1.0 / sum(factors[i] * r_.ld[i] for i in range(NB))
        o = jnp.zeros((R, D), F32)
        for i in range(NB):
            r_.rb[l, i] = factors[i] * inv
            o = o + factors[i] * inv * r_.od[i]
        r_.oraw[l] = o
        ob = o.astype(BF16)
        r_.ob[l] = ob
        t1 = r_.xf[l] + dot(ob, r_.wo[l])
        r_.z1[l] = t1
        mean1 = col_sum(t1) / R
        return mean1, col_sum((t1 - mean1) * (t1 - mean1))

    def convolution(l):
        xs = r_.xs
        xb = xs[l, me]
        r_.xe[l, 0:R] = xb
        r_.xe[l, R : R + 32] = dot(r_.HP[...], xs[l, prev]).astype(BF16)
        r_.xe[l, R + 32 : R + 64] = dot(r_.HN[...], xs[l, nxt]).astype(BF16)
        xe = r_.xe[l]
        made = dot(xe, r_.wp[l])
        pd_high, pd_low = split(made[:, 2 * D : 3 * D])
        r_.re[0:256] = made[:, 3 * D :].astype(BF16)
        r_.re[256:512] = r_.we[l]
        r_.re[512:768] = pd_high
        r_.re[768:1024] = pd_low
        r_.gate[l] = dot(r_.le[...], r_.re[...])
        r_.bs[l] = dot(r_.le[:, 0:256], made[:, D : 2 * D].astype(BF16)).astype(BF16)
        for at in range(0, E, 64):
            here = slice(at, at + 64)
            gate = sigmoid(r_.gate[l, here])
            r_.gate[l, here] = gate
            high, low = split(jnp.concatenate([gate * r_.bs[l, here].astype(F32), gate], 1))
            r_.gg[here] = high
            r_.gg[E + at : E + at + 64] = low
        num_den = dot(r_.TT[...], r_.gg[...])
        pa, num, den = made[0:R, 0:D], num_den[:, 0:D], num_den[:, D:]
        r_.num[l] = num
        r_.den[l] = den
        msg = pa + num / (den + GATE_EPS)
        r_.z0[l] = msg
        mean0 = col_sum(msg) / R
        sync_start(3 * l, mean0, col_sum((msg - mean0) * (msg - mean0)))

    def forward(l, carry):
        def ready(js):
            for j in js:
                moved = (r_.gb[l, j].astype(F32) + r_.moff[j, 0:1]) * r_.move[0:1] + r_.move[1:2]
                r_.xs[l, j] = moved.astype(BF16)

        r_.xs[l, me] = r_.xf[l].astype(BF16)
        prepare_queries(l)
        arrive(r_.gb.at[l, 2 * z_from(1) + par], r_.agc_r.at[l, 1])
        gather_take(l, 0)
        gather_take(l, 1)
        ready([partner, 2 * z_from(1) + par, 2 * z_from(1) + 1 - par])

        def middle(i, hf):
            when((i == 0) & (hf == 0), *[functools.partial(gather_pass, l, t) for t in range(2, NZ)])

        def block(i, carry):
            attention_block(l, i, middle)

            @pl.when(i == 0)
            def _():
                for t in range(2, NZ):
                    gather_take(l, t)
                ready([2 * z_from(t) + p for t in range(2, NZ) for p in range(2)])
                convolution(l)

            return carry

        lax.fori_loop(0, NB, block, 0)
        mean1, sq1 = attention_end(l)
        sync_start(3 * l + 1, mean1, sq1)
        mean0, sq0 = sync_moments(3 * l)
        inv0 = lax.rsqrt(sq0 / total + NORM_EPS)
        r_.iv[l, 0:1] = inv0
        z0 = (r_.z0[l] - mean0) * inv0
        r_.z0[l] = z0
        n0 = z0 * r_.gain[l, 0:1] + r_.shift[l, 0:1]
        r_.local[...] = r_.xf[l] + n0 * sigmoid(n0)
        mean1, sq1 = sync_moments(3 * l + 1)
        inv1 = lax.rsqrt(sq1 / total + NORM_EPS)
        r_.iv[l, 1:2] = inv1
        z1 = (r_.z1[l] - mean1) * inv1
        r_.z1[l] = z1
        mix = r_.local[...] + z1 * r_.gain[l, 1:2] + r_.shift[l, 1:2]
        mb = mix.astype(BF16)
        r_.mb[l] = mb
        u = dot(mb, r_.wu[l])
        r_.u[l] = u
        g = (u * sigmoid(u)).astype(BF16)
        r_.g[l] = g
        y = mix + dot(g, r_.wd[l])
        r_.z2[l] = y
        mean = col_sum(y) / R
        cent = y - mean
        k = 3 * l + 2
        sync_start(k, mean, col_sum(cent * cent))

        @pl.when(l < L - 1)
        def _():
            r_.gb[l + 1, me] = cent.astype(BF16)
            gather_start(l + 1)

        @pl.when(l == L - 1)
        def _():
            dy = r_.cot[...].astype(F32)
            sync_start(3 * L, col_sum(dy), col_sum(dy * cent))

        tot_mean, tot_sq = sync_moments(k)
        inv2 = lax.rsqrt(tot_sq / total + NORM_EPS)
        r_.iv[l, 2:3] = inv2
        z2 = (r_.z2[l] - tot_mean) * inv2
        r_.z2[l] = z2
        gain, shift = r_.gain[l, 2:3], r_.shift[l, 2:3]
        r_.xf[l + 1] = z2 * gain + shift

        @pl.when(l == L - 1)
        def _():
            sync_wait(3 * L)
            sums, means = r_.st1[3 * L], r_.st1[k][:, 0:2]
            mean = jnp.mean(means, 0)
            dy_sum = jnp.sum(sums[:, 0:2], 0)
            dy_cent = jnp.sum(sums[:, 2:4] + (means - mean) * sums[:, 0:2], 0)
            dy_sum, dy_cent = unpack(jnp.concatenate([dy_sum, dy_cent], 0))
            r_.gshift[l, 2:3] = dy_sum
            r_.ggain[l, 2:3] = dy_cent * inv2

        for j in range(N):
            tile = r_.st1[k, rep * N + j]
            r_.moff[j, 0:1] = jnp.concatenate([tile[0:1], tile[1:2]], 1) - tot_mean
        r_.move[0:1] = inv2 * gain
        r_.move[1:2] = shift
        return carry

    lax.fori_loop(0, L, forward, 0)
    act_copy = pltpu.make_async_copy(r_.xf.at[L], r_.out_act, r_.store.at[0])
    act_copy.start()

    def back_feed_forward(l, k):
        s2, g2 = r_.gshift[l, 2:3], r_.ggain[l, 2:3]
        d3 = r_.gain[l, 2:3] * r_.iv[l, 2:3] * (r_.dy[...] - s2 / total - r_.z2[l] * (g2 / total))
        db = d3.astype(BF16)
        dub = (dot_nt(db, r_.wd[l]) * silu_slope(r_.u[l])).astype(BF16)
        dmix = d3 + dot_nt(dub, r_.wu[l])
        r_.dmix[...] = dmix
        n0 = r_.z0[l] * r_.gain[l, 0:1] + r_.shift[l, 0:1]
        gy0 = dmix * silu_slope(n0)
        sync_start(k, col_sum(dmix), col_sum(dmix * r_.z1[l]))
        sync_start(k + 1, col_sum(gy0), col_sum(gy0 * r_.z0[l]))
        r_.gy0[...] = gy0
        at = put(r_.gs_early, l, 512, dot_tn(r_.mb[l], dub))
        put(r_.gs_early, l, at, dot_tn(r_.g[l], db))
        r_.vT[...] = r_.vv[l].T
        r_.xeT[...] = r_.xe[l].T
        for hf in range(2):
            r_.qmT[hf] = r_.qm[l, hf].T

    def back_norms(l, k):
        s1, g1 = sync_sums(k)
        r_.gshift[l, 1:2] = s1
        r_.ggain[l, 1:2] = g1
        dmix = r_.dmix[...]
        d2 = r_.gain[l, 1:2] * r_.iv[l, 1:2] * (dmix - s1 / total - r_.z1[l] * (g1 / total))
        dab = d2.astype(BF16)
        r_.dxo[...] = dmix + d2
        r_.dob[...] = dot_nt(dab, r_.wo[l]).astype(BF16).astype(F32)
        put(r_.gs_early, l, 0, dot_tn(r_.ob[l], dab))
        r_.gkv[...] = jnp.zeros((2 * D, D), F32)
        r_.dq[...] = jnp.zeros((R, D), F32)

    def back_attention_block(l, i, between):
        t1 = (i + 1) % NB
        half = (zh + t1) % NB
        rows = pl.ds(pl.multiple_of(half * W, 128), W)

        def heads(hf, carry):
            lanes = lane_half(hf)
            dos = r_.dob[:, lanes] * r_.rb[l, (NB - t1) % NB, :, lanes]
            prod = dos * r_.oraw[l, :, lanes]
            for k in range(HK):
                r_.dom[k * R : (k + 1) * R, 0:128] = jnp.where(lane_head == k, dos, 0.0).astype(BF16)
                r_.dom[k * R : (k + 1) * R, 128:256] = jnp.where(lane_head == k, -prod, 0.0).astype(BF16)
            parts = []
            right = jnp.concatenate([r_.vT[lanes, rows], jnp.ones((128, W), BF16)], 0)
            for c in range(HK // 2):
                both = slice(2 * c * R, 2 * (c + 1) * R)
                r_.sc[c % 2, 0 : 2 * R] = dot(r_.dom[both], right)
                for k in range(2):
                    for at in range(0, R, STRIP):
                        first = pl.multiple_of((hf * HK + 2 * c + k) * R + at, STRIP)
                        e = r_.pst[l, pl.ds(first, STRIP), rows].astype(F32)
                        ds = e * r_.sc[c % 2, k * R + at : k * R + at + STRIP]
                        r_.dss[(2 * c + k) * R + at : (2 * c + k) * R + at + STRIP] = ds.astype(BF16)
                part = dot(r_.dss[both], r_.kk[l, rows, lanes])
                parts += [part[0:R], part[R : 2 * R]]
            r_.dq[:, lanes] += by_head(parts)
            dk = dot(r_.qmT[hf], r_.dss[...]) * scale
            r_.dkv[pl.ds(pl.multiple_of(hf * 128, 128), 128)] = dk.astype(BF16)
            dv = dot(r_.dom[:, 0:128].T, r_.pst[l, head_rows(hf, 0, HK), rows])
            r_.dkv[pl.ds(pl.multiple_of(D + hf * 128, 128), 128)] = dv.astype(BF16)
            between(i, hf)
            return carry

        lax.fori_loop(0, 2, heads, 0)
        dx = dot(r_.wqkv[l, :, D:], r_.dkv[...]).T
        r_.dxs[l, pl.ds(2 * half, 2)] = dx.astype(BF16).reshape(2, 2, R, D)

        @pl.when(i < NB - 1)
        def _():
            for low in range(2):
                zb = 2 * half + low
                send_rows(r_.dxs.at[l, zb, 1 - par], r_.rs1.at[l, zb], R,
                     r_.rsp_s.at[l, 2 * i + low], r_.rsp_r.at[l, 2 * i + low], nodes=partner)

        @pl.when(i == NB - 1)
        def _():
            near = z_to(1)
            send_rows(r_.dxs.at[l, z, 1 - par], r_.ro.at[l, 0], R, r_.ro_s.at[l, 0], r_.ro_r.at[l, 0], nodes=partner)
            send_rows(r_.dxs.at[l, near, par], r_.ro.at[l, 1], R, r_.ro_s.at[l, 1], r_.ro_r.at[l, 1], nodes=2 * near + par)
            send_rows(r_.dxs.at[l, near, 1 - par], r_.ro.at[l, 2], R, r_.ro_s.at[l, 2], r_.ro_r.at[l, 2],
                 nodes=2 * near + 1 - par)

        r_.gkv[...] += dot(r_.dkv[...], r_.xs[l, pl.ds(4 * half, 4)].reshape(W, D))

    def pass_on(l, i, t):
        zb = z_to(t)
        arrive(r_.rs1.at[l, zb], r_.rsp_r.at[l, 2 * i + zb % 2])
        both = r_.dxs[l, zb, par].astype(F32) + r_.rs1[l, zb].astype(F32)
        r_.cs[l, zb] = both.astype(BF16)
        send_rows(r_.cs.at[l, zb], r_.rs2.at[l, z], R, r_.rsc_s.at[l, t], r_.rsc_r.at[l, t], nodes=2 * zb + par)

    def back_convolution(l, k):
        s0, g0 = sync_sums(k + 1)
        r_.gshift[l, 0:1] = s0
        r_.ggain[l, 0:1] = g0
        inv_den = 1.0 / (r_.den[l] + GATE_EPS)
        dm = r_.gain[l, 0:1] * r_.iv[l, 0:1] * (r_.gy0[...] - s0 / total - r_.z0[l] * (g0 / total))
        dnum = dm * inv_den
        dden = -dnum * r_.num[l] * inv_den
        high, low = split(jnp.concatenate([dnum, dden], 1))
        r_.dn[0:R] = high
        r_.dn[256 : 256 + R] = low
        r_.sc[0, 0:E, 0 : 2 * D] = dot(r_.le[:, 512:1024], r_.dn[...])
        for at in range(0, E, 64):
            here = slice(at, at + 64)
            gate, dnum_e = r_.gate[l, here], r_.sc[0, here, 0:D]
            dgp = (dnum_e * r_.bs[l, here].astype(F32) + r_.sc[0, here, D : 2 * D]) * gate * (1.0 - gate)
            r_.gg[here, 0:D] = (dnum_e * gate).astype(BF16)
            r_.gg[here, D:] = dgp.astype(BF16)
        ext = dot(r_.ST[...], r_.gg[0:E]).astype(BF16)
        r_.dproj[0:R, 0:D] = dm.astype(BF16)
        r_.dproj[:, D : 2 * D] = ext[:, 0:D]
        r_.dproj[0:R, 2 * D : 3 * D] = dot(r_.TT[:, 0:E], r_.gg[0:E, D:]).astype(BF16)
        r_.dproj[:, 3 * D :] = ext[:, D:]
        dxe = dot_nt(r_.dproj[...], r_.wp[l])
        r_.hs[l, 0] = dxe[R : R + 32].astype(BF16)
        r_.hs[l, 1] = dxe[R + 32 : R + 64].astype(BF16)
        send(r_.hs.at[l, 0], r_.hr.at[l, 1], r_.hal_s.at[l, 0], r_.hal_r.at[l, 0], nodes=prev)
        send(r_.hs.at[l, 1], r_.hr.at[l, 0], r_.hal_s.at[l, 1], r_.hal_r.at[l, 1], nodes=nxt)
        r_.dxo[...] += dxe[0:R]

    def conv_weight_grads(l):
        at = put(r_.gs_conv, l, 0, dot(r_.xeT[...], r_.dproj[...]))
        put(r_.gs_conv, l, at, dot(r_.efT[...], r_.gg[0:E, D:]))

    def back_input(l):
        dx = r_.dxo[...]
        dx = dx + r_.dxs[l, z, par].astype(F32)
        for slot in range(3):
            arrive(r_.ro.at[l, slot], r_.ro_r.at[l, slot])
            dx = dx + r_.ro[l, slot].astype(F32)
        for t in range(2, NZ):
            c = z_from(t)
            arrive(r_.rs2.at[l, c], r_.rsc_r.at[l, t])
            dx = dx + r_.rs2[l, c].astype(F32)
        arrive(r_.hr.at[l, 0], r_.hal_r.at[l, 1])
        arrive(r_.hr.at[l, 1], r_.hal_r.at[l, 0])
        back = jnp.concatenate(
            [r_.hr[l, 0].astype(F32)[0:24], r_.hr[l, 1].astype(F32)[0:24], jnp.zeros((16, D), F32)], 0
        )
        return dx + dot(r_.A[...], back.astype(BF16))

    r_.dy[...] = r_.cot[...].astype(F32)

    E1, C1, Q1, E0, C0, Q0 = range(len(GROUPS))

    def steps(*pairs):
        return [functools.partial(reduce_step, g, k) for g, k in pairs]

    r_.dy[...] = r_.cot[...].astype(F32)

    def backward(b, carry):
        l = L - 1 - b
        first, last = b == 0, b == L - 1
        k = 3 * L + 1 + 2 * b
        conv = functools.partial(back_convolution, l, k)
        conv_grads = functools.partial(conv_weight_grads, l)
        back_feed_forward(l, k)
        back_norms(l, k)
        when(first, *steps((E1, 0)))
        when(last, *steps((E1, 3), (C1, 1), (Q1, 1), (E0, 0)), conv, conv_grads,
             *steps((C1, 2), (Q1, 2), (E1, 4), (E0, 1), (C0, 0)))

        def between(i, hf):
            when(first & (i == 0) & (hf == 0), *steps((E1, 1)))
            when(first & (i == 1) & (hf == 0), *steps((E1, 2)))
            when(last & (i == 0) & (hf == 0), *steps((C0, 1)))
            when(last & (i == 0) & (hf == 1), *steps((E0, 2), (C1, 3), (Q1, 3), (E1, 5)))
            when(last & (i == 1) & (hf == 0), *steps((E0, 3), (C0, 2), (C1, 4), (Q1, 4), (E1, 6)))
            when(last & (i == 1) & (hf == 1), *steps((E0, 4), (C1, 5), (Q1, 5)))
            for t in range(2, NZ):
                when((i == 1) & (hf == 0), functools.partial(pass_on, l, 0, t))

        def block(i, carry):
            back_attention_block(l, i, between)
            return carry

        lax.fori_loop(0, NB, block, 0)
        when(first, conv)
        dqb = (r_.dq[...] * scale).astype(BF16)
        r_.dxo[...] += dot_nt(dqb, r_.wqkv[l, :, 0:D])
        when(first, conv_grads, *steps((C1, 0)))
        at = put(r_.gs_qkv, l, 0, dot(r_.xeT[:, 0:R], dqb))
        put(r_.gs_qkv, l, at, r_.gkv[...].T)

        @pl.when(first)
        def _():
            dx = back_input(l)
            r_.dy[...] = dx
            below = L - 2
            sync_start(SYNCS - 1, col_sum(dx), col_sum(dx * r_.z2[below]))
            reduce_step(Q1, 0)
            s2, g2 = sync_sums(SYNCS - 1)
            r_.gshift[below, 2:3] = s2
            r_.ggain[below, 2:3] = g2

        return carry

    lax.fori_loop(0, L, backward, 0)
    for step in steps((Q0, 0), (C0, 3), (E0, 5), (C1, 6), (Q1, 6), (Q0, 1)):
        step()
    r_.dy[...] = back_input(0)
    in_copy = pltpu.make_async_copy(r_.dy, r_.grad_in, r_.store.at[1])
    in_copy.start()
    for step in steps(
        (C0, 4), (E0, 6), (C1, 7), (Q0, 2),
        (C0, 5), (E0, 7), (C1, 8), (Q0, 3),
        (C0, 6), (E0, 8), (Q0, 4),
    ):
        step()
    for l in range(L):
        for k in range(3):
            r_.ggain_out[k, l : l + 1] = r_.ggain[l, k : k + 1]
            r_.gshift_out[k, l : l + 1] = r_.gshift[l, k : k + 1]
    for g in range(len(GROUPS)):
        reduce_drain(g)
    sent(r_.meta.at[0 : N - 1], r_.meta_s.at[0])
    for k in range(SYNCS):
        sent(r_.st1.at[k, 0 : M * N - 1], r_.st1_s.at[k])
    for l in range(L):
        for t in range(NZ):
            sent(r_.gb.at[l, 0], r_.agp_s.at[l, t])
            if t > 0:
                sent(r_.gb.at[l, 0], r_.agc_s.at[l, t])
            if t > 1:
                sent(r_.rs1.at[l, 0], r_.rsc_s.at[l, t])
        for slot in range(2 * (NB - 1)):
            sent(r_.rs1.at[l, 0], r_.rsp_s.at[l, slot])
        for slot in range(3):
            sent(r_.ro.at[l, 0], r_.ro_s.at[l, slot])
        for side in range(2):
            sent(r_.hs.at[l, 0], r_.hal_s.at[l, side])
    act_copy.wait()
    in_copy.wait()


def finish_kernel(act_h, gin_h, *refs):
    n = len(GROUPS)
    held, (ggain_h, gshift_h), refs = refs[:n], refs[n : n + 2], refs[n + 2 :]
    act_o, gin_o, proj_o, edge_o, qkv_o, out_o, up_o, down_o, ggain_o, gshift_o = refs[:10]
    summed, refs = refs[10 : 10 + n], refs[10 + n :]
    act, gin, proj, edge, qkv, out, up, down, in_sem, out_sem = refs
    loads = [
        pltpu.make_async_copy(src, dst, in_sem.at[i])
        for i, (src, dst) in enumerate(zip(held + (act_h, gin_h), summed + (act, gin), strict=True))
    ]
    for load in loads:
        load.start()
    ggain_o[...] = ggain_h[...]
    gshift_o[...] = gshift_h[...]
    stores = []

    def store(src, dst):
        copy = pltpu.make_async_copy(src, dst, out_sem.at[len(stores)])
        copy.start()
        stores.append(copy)

    def widen(dst, l, g, at, first=0, last=None):
        rows = dst.shape[1]
        for c in range(first, dst.shape[2] // 128 if last is None else last):
            dst[l, :, 128 * c : 128 * (c + 1)] = summed[g][at : at + rows].astype(F32)
            at += rows
        return at

    for g, (name, l, first, rows, _) in enumerate(GROUPS):
        loads[g].wait()
        if name == "early":
            at = widen(out, l, g, 0)
            store(out.at[l], out_o.at[l])
            at = widen(up, l, g, at)
            store(up.at[l], up_o.at[l])
            widen(down, l, g, at)
            store(down.at[l], down_o.at[l])
        elif name == "conv":
            at = widen(proj, l, g, 0)
            store(proj.at[l], proj_o.at[l])
            widen(edge, l, g, at)
            store(edge.at[l], edge_o.at[l])
        else:
            widen(qkv, l, g, 0, first // 256, (first + rows) // 256)
            if first + rows == 1536:
                store(qkv.at[l], qkv_o.at[l])
    for i, (src, dst) in enumerate(((act, act_o), (gin, gin_o))):
        loads[n + i].wait()
        store(src, dst)
    for copy in stores:
        copy.wait()


def fused_device(
    N, M, node_input, edge_feat, graph_ids, edge_src, edge_dst, halo_send, w_proj, w_edge, w_qkv,
    w_out, w_up, w_down, norm_gain, norm_shift, cotangent,
):
    R, D = node_input.shape
    E = edge_feat.shape[0]
    L = w_proj.shape[0]
    names = scratch_list(N, M, L, R, E)
    vmem = pl.BlockSpec(memory_space=pltpu.VMEM)
    hbm = pl.BlockSpec(memory_space=pltpu.HBM)
    shape = jax.ShapeDtypeStruct
    rows = shape((R, D), F32)
    norm = shape((3, L, D), F32)
    groups = [shape((rows_g, 128), BF16) for _, _, _, rows_g, _ in GROUPS]
    outs = pl.pallas_call(
        functools.partial(kernel, N, M, L, tuple(names)),
        out_shape=[rows, rows, *groups, norm, norm],
        in_specs=[hbm] + [vmem] * 4 + [hbm] * 7 + [vmem] * 2 + [hbm],
        out_specs=[hbm] * (2 + len(GROUPS)) + [vmem] * 2,
        scratch_shapes=list(names.values()),
        compiler_params=pltpu.CompilerParams(
            collective_id=0, has_side_effects=True, vmem_limit_bytes=60 << 20
        ),
        name="layers",
    )(node_input, graph_ids, edge_src, edge_dst, halo_send, edge_feat, w_proj, w_edge, w_qkv, w_out, w_up,
      w_down, norm_gain.transpose(1, 0, 2), norm_shift.transpose(1, 0, 2), cotangent)
    weights = [shape(w.shape, F32) for w in (w_proj, w_edge, w_qkv, w_out, w_up, w_down)]
    results = pl.pallas_call(
        finish_kernel,
        out_shape=[rows, rows, *weights, norm, norm],
        in_specs=[hbm] * (2 + len(GROUPS)) + [vmem] * 2,
        out_specs=[hbm] * 8 + [vmem] * 2,
        scratch_shapes=[pltpu.VMEM(s.shape, s.dtype) for s in (*groups, rows, rows, *weights)]
        + [pltpu.SemaphoreType.DMA((len(GROUPS) + 2,)), pltpu.SemaphoreType.DMA((14,))],
        compiler_params=pltpu.CompilerParams(vmem_limit_bytes=60 << 20),
        name="gradients",
    )(*outs)
    ggain, gshift = results[8].transpose(1, 0, 2), results[9].transpose(1, 0, 2)
    return (*results[:8], ggain, gshift)


BLOCK_CAP = 2048


def extended_2(block, sides, width):
    for axis, dim in sides:
        count = lax.axis_size(axis)
        forward = [(i, i + 1) for i in range(count - 1)]
        forward.append((count - 1, 0))
        backward = [(target, source) for source, target in forward]
        low = lax.ppermute(
            lax.slice_in_dim(block, block.shape[dim] - width, None, axis=dim), axis, forward
        )
        high = lax.ppermute(lax.slice_in_dim(block, 0, width, axis=dim), axis, backward)
        block = jnp.concatenate([low, block, high], axis=dim)
    return block


def block_length(total_rows, upper_limit):
    for length in range(min(total_rows, upper_limit), 0, -1):
        if total_rows % length == 0:
            return length
    return 1


def outer_product(left, right):
    return lax.dot_general(
        left, right, (((0,), (0,)), ((), ())), preferred_element_type=jnp.float32
    )


def times_transposed(left, weight):
    return lax.dot_general(
        left, weight, (((1,), (1,)), ((), ())), preferred_element_type=jnp.float32
    )


def forward_product(left, weight):
    return jnp.dot(left, weight, preferred_element_type=jnp.float32)


def silu_slope_plain(inputs):
    logistic = jax.nn.sigmoid(inputs)
    return logistic * (1.0 + inputs * (1.0 - logistic))


def normalize(inputs, gain_row, shift_row, node_total):
    batch_mean = lax.psum(jnp.sum(inputs, 0), ("nodes", "rep")) / node_total
    centred = inputs - batch_mean
    batch_var = lax.psum(jnp.sum(centred * centred, 0), ("nodes", "rep")) / node_total
    inv_std = lax.rsqrt(batch_var + NORM_EPS)
    standard = (inputs - batch_mean) * inv_std
    return (standard * gain_row + shift_row, standard, inv_std)


def normalize_back(grad_out, standard, inv_std, gain_row, node_total):
    shift_grad, gain_grad = lax.psum(
        (jnp.sum(grad_out, 0), jnp.sum(grad_out * standard, 0)), ("nodes", "rep")
    )
    grad_in = (
        gain_row
        * inv_std
        * (grad_out - shift_grad / node_total - standard * gain_grad / node_total)
    )
    return (grad_in, gain_grad, shift_grad)


def exchange_sources(outgoing):
    halo_rows = outgoing.shape[0] // 2
    grown = extended_2(outgoing, (("nodes", 0),), halo_rows)
    return jnp.concatenate([grown[:halo_rows], grown[3 * halo_rows :]], 0)


def return_sources(incoming_grad):
    halo_rows = incoming_grad.shape[0] // 2
    grown = extended_2(incoming_grad.astype(jnp.bfloat16), (("nodes", 0),), halo_rows).astype(
        incoming_grad.dtype
    )
    return jnp.concatenate([grown[:halo_rows], grown[3 * halo_rows :]], 0)


def attend_forward(query_rows, key_rows, value_rows, local_graphs, group_graphs):
    row_count = query_rows.shape[0]
    score_scale = HEAD_DIM ** (-0.5)
    queries = query_rows.reshape(row_count, HEADS, HEAD_DIM)

    def add_piece(carried, kv_piece, first_row):
        key_piece, value_piece = kv_piece
        piece_rows = key_piece.shape[0]
        block_len = block_length(piece_rows, BLOCK_CAP)

        def add_block(block_state, block_index):
            row_max, row_sum, accumulated = block_state
            block_start = block_index * block_len
            key_block = lax.dynamic_slice_in_dim(key_piece, block_start, block_len, 0).reshape(
                block_len, HEADS, HEAD_DIM
            )
            value_block = lax.dynamic_slice_in_dim(value_piece, block_start, block_len, 0).reshape(
                block_len, HEADS, HEAD_DIM
            )
            key_graphs = lax.dynamic_slice_in_dim(
                group_graphs, first_row + block_start, block_len, 0
            )
            same_graph = (local_graphs[:, None] == key_graphs[None, :])[None]
            scores = (
                jnp.einsum("qhd,khd->hqk", queries, key_block, preferred_element_type=jnp.float32)
                * score_scale
            )
            scores = jnp.where(same_graph, scores, NEG)
            new_max = jnp.maximum(row_max, jnp.max(scores, 2))
            weights = jnp.where(same_graph, jnp.exp(scores - new_max[:, :, None]), 0.0)
            factor = jnp.exp(row_max - new_max)
            row_sum = row_sum * factor + jnp.sum(weights, 2)
            contrib = jnp.einsum(
                "hqk,khd->qhd",
                weights.astype(jnp.bfloat16),
                value_block,
                preferred_element_type=jnp.float32,
            )
            accumulated = accumulated * jnp.transpose(factor)[:, :, None] + contrib
            return ((new_max, row_sum, accumulated), None)

        carried, _ = lax.scan(add_block, carried, jnp.arange(piece_rows // block_len))
        return carried

    start_state = (
        jnp.full((HEADS, row_count), NEG, jnp.float32),
        jnp.zeros((HEADS, row_count), jnp.float32),
        jnp.zeros((row_count, HEADS, HEAD_DIM), jnp.float32),
    )
    row_max, row_sum, accumulated = add_piece(
        start_state,
        (
            lax.all_gather(key_rows, "nodes", axis=0, tiled=True),
            lax.all_gather(value_rows, "nodes", axis=0, tiled=True),
        ),
        jnp.int32(0),
    )
    attn_raw = accumulated / jnp.transpose(row_sum)[:, :, None]
    log_sum = row_max + jnp.log(row_sum)
    return (attn_raw, log_sum)


def attend_backward(
    query_rows, key_rows, value_rows, grad_low, attn_raw, log_sum, local_graphs, group_graphs
):
    row_count = query_rows.shape[0]
    model_width = HEADS * HEAD_DIM
    score_scale = HEAD_DIM ** (-0.5)
    queries = query_rows.reshape(row_count, HEADS, HEAD_DIM)
    grad_heads = grad_low.reshape(row_count, HEADS, HEAD_DIM)
    row_delta = jnp.einsum("qhd,qhd->hq", grad_heads.astype(jnp.float32), attn_raw)

    def score_block(key_block, value_block, key_graphs):
        same_graph = (local_graphs[:, None] == key_graphs[None, :])[None]
        scores = (
            jnp.einsum("qhd,khd->hqk", queries, key_block, preferred_element_type=jnp.float32)
            * score_scale
        )
        attn_weights = jnp.exp(jnp.where(same_graph, scores - log_sum[:, :, None], NEG))
        grad_weights = jnp.einsum(
            "qhd,khd->hqk", grad_heads, value_block, preferred_element_type=jnp.float32
        )
        grad_scores = (attn_weights * (grad_weights - row_delta[:, :, None])).astype(jnp.bfloat16)
        return (attn_weights, grad_scores)

    def key_terms(attn_weights, grad_scores, block_len):
        grad_keys = (
            jnp.einsum("hqk,qhd->khd", grad_scores, queries, preferred_element_type=jnp.float32)
            * score_scale
        )
        grad_values = jnp.einsum(
            "hqk,qhd->khd",
            attn_weights.astype(jnp.bfloat16),
            grad_heads,
            preferred_element_type=jnp.float32,
        )
        return jnp.concatenate(
            [
                grad_keys.reshape(block_len, model_width),
                grad_values.reshape(block_len, model_width),
            ],
            1,
        )

    def query_term(grad_scores, key_block):
        return (
            jnp.einsum("hqk,khd->qhd", grad_scores, key_block, preferred_element_type=jnp.float32)
            * score_scale
        )

    group_rows = group_graphs.shape[0]

    def add_piece(carried, kv_piece, first_row):
        key_piece, value_piece = kv_piece
        piece_rows = key_piece.shape[0]
        block_len = block_length(piece_rows, BLOCK_CAP)

        def add_block(block_state, block_index):
            grad_query, buffer = block_state
            block_start = block_index * block_len
            key_block = lax.dynamic_slice_in_dim(key_piece, block_start, block_len, 0).reshape(
                block_len, HEADS, HEAD_DIM
            )
            value_block = lax.dynamic_slice_in_dim(value_piece, block_start, block_len, 0).reshape(
                block_len, HEADS, HEAD_DIM
            )
            place = first_row + block_start
            key_graphs = lax.dynamic_slice_in_dim(group_graphs, place, block_len, 0)
            attn_weights, grad_scores = score_block(key_block, value_block, key_graphs)
            grad_query = grad_query + query_term(grad_scores, key_block)
            block_terms = key_terms(attn_weights, grad_scores, block_len)
            current = lax.dynamic_slice_in_dim(buffer, place, block_len, 0)
            buffer = lax.dynamic_update_slice_in_dim(buffer, current + block_terms, place, 0)
            return ((grad_query, buffer), None)

        carried, _ = lax.scan(add_block, carried, jnp.arange(piece_rows // block_len))
        return carried

    start_state = (
        jnp.zeros((row_count, HEADS, HEAD_DIM), jnp.float32),
        jnp.zeros((group_rows, 2 * model_width), jnp.float32),
    )
    grad_query, buffer = add_piece(
        start_state,
        (
            lax.all_gather(key_rows, "nodes", axis=0, tiled=True),
            lax.all_gather(value_rows, "nodes", axis=0, tiled=True),
        ),
        jnp.int32(0),
    )
    grad_kv = lax.psum_scatter(buffer, "nodes", scatter_dimension=0, tiled=True)
    return (
        grad_query.reshape(row_count, model_width),
        grad_kv[:, :model_width],
        grad_kv[:, model_width:],
    )


def layer_forward(
    hidden, params, edge_feat, edge_src, edge_dst, halo_send, local_graphs, group_graphs, node_total
):
    w_proj, w_edge, w_qkv, w_out, w_up, w_down, norm_gains, norm_shifts = params
    row_count, model_width = hidden.shape
    hidden_low = hidden.astype(jnp.bfloat16)
    projected = forward_product(hidden_low, w_proj)
    self_term = projected[:, :model_width]
    dest_term = projected[:, 2 * model_width : 3 * model_width]
    source_rows = jnp.concatenate(
        [projected[:, model_width : 2 * model_width], projected[:, 3 * model_width :]], 1
    ).astype(jnp.bfloat16)
    incoming = exchange_sources(source_rows[halo_send])
    extended = jnp.concatenate([source_rows, incoming], 0)
    edge_rows = extended[edge_src].astype(jnp.float32)
    source_b = edge_rows[:, :model_width]
    source_e = edge_rows[:, model_width:]
    edge_proj = forward_product(edge_feat, w_edge)
    gating = jax.nn.sigmoid(dest_term[edge_dst] + source_e + edge_proj)
    numerator = jax.ops.segment_sum(gating * source_b, edge_dst, row_count)
    denominator = jax.ops.segment_sum(gating, edge_dst, row_count)
    message = self_term + numerator / (denominator + GATE_EPS)
    normed_one, standard_one, inv_one = normalize(
        message, norm_gains[0], norm_shifts[0], node_total
    )
    local_out = hidden + jax.nn.silu(normed_one)
    qkv_low = forward_product(hidden_low, w_qkv).astype(jnp.bfloat16)
    query_rows = qkv_low[:, :model_width]
    key_rows = qkv_low[:, model_width : 2 * model_width]
    value_rows = qkv_low[:, 2 * model_width :]
    attn_raw, log_sum = attend_forward(query_rows, key_rows, value_rows, local_graphs, group_graphs)
    attn_low = attn_raw.reshape(row_count, model_width).astype(jnp.bfloat16)
    attn_proj = forward_product(attn_low, w_out)
    normed_two, standard_two, inv_two = normalize(
        hidden + attn_proj, norm_gains[1], norm_shifts[1], node_total
    )
    mixed = local_out + normed_two
    mixed_low = mixed.astype(jnp.bfloat16)
    up_proj = forward_product(mixed_low, w_up)
    activated = jax.nn.silu(up_proj).astype(jnp.bfloat16)
    down_proj = forward_product(activated, w_down)
    normed_three, standard_three, inv_three = normalize(
        mixed + down_proj, norm_gains[2], norm_shifts[2], node_total
    )
    saved = (
        hidden_low,
        source_b,
        gating,
        numerator,
        denominator,
        normed_one,
        standard_one,
        inv_one,
        query_rows,
        key_rows,
        value_rows,
        attn_raw,
        log_sum,
        attn_low,
        standard_two,
        inv_two,
        mixed_low,
        up_proj,
        activated,
        standard_three,
        inv_three,
    )
    return (normed_three, saved)


def layer_backward(
    grad_out,
    params,
    saved,
    edge_feat,
    edge_src,
    edge_dst,
    halo_send,
    local_graphs,
    group_graphs,
    node_total,
):
    w_proj, w_edge, w_qkv, w_out, w_up, w_down, norm_gains, norm_shifts = params
    (
        hidden_low,
        source_b,
        gating,
        numerator,
        denominator,
        normed_one,
        standard_one,
        inv_one,
        query_rows,
        key_rows,
        value_rows,
        attn_raw,
        log_sum,
        attn_low,
        standard_two,
        inv_two,
        mixed_low,
        up_proj,
        activated,
        standard_three,
        inv_three,
    ) = saved
    row_count, model_width = grad_out.shape
    grad_three, gain_three, shift_three = normalize_back(
        grad_out, standard_three, inv_three, norm_gains[2], node_total
    )
    down_grad = grad_three.astype(jnp.bfloat16)
    grad_w_down = outer_product(activated, down_grad)
    up_grad = (times_transposed(down_grad, w_down) * silu_slope_plain(up_proj)).astype(jnp.bfloat16)
    grad_w_up = outer_product(mixed_low, up_grad)
    grad_mixed = grad_three + times_transposed(up_grad, w_up)
    grad_two, gain_two, shift_two = normalize_back(
        grad_mixed, standard_two, inv_two, norm_gains[1], node_total
    )
    out_grad = grad_two.astype(jnp.bfloat16)
    grad_w_out = outer_product(attn_low, out_grad)
    attn_grad = times_transposed(out_grad, w_out).astype(jnp.bfloat16)
    grad_query, grad_key, grad_value = attend_backward(
        query_rows, key_rows, value_rows, attn_grad, attn_raw, log_sum, local_graphs, group_graphs
    )
    qkv_grad = jnp.concatenate([grad_query, grad_key, grad_value], 1).astype(jnp.bfloat16)
    grad_w_qkv = outer_product(hidden_low, qkv_grad)
    grad_message, gain_one, shift_one = normalize_back(
        grad_mixed * silu_slope_plain(normed_one), standard_one, inv_one, norm_gains[0], node_total
    )
    shifted = denominator + GATE_EPS
    grad_numer = grad_message / shifted
    grad_denom = -grad_message * numerator / (shifted * shifted)
    numer_edge = grad_numer[edge_dst]
    grad_gate = numer_edge * source_b + grad_denom[edge_dst]
    grad_pre_edge = grad_gate * gating * (1.0 - gating)
    edge_grad = grad_pre_edge.astype(jnp.bfloat16)
    grad_w_edge = outer_product(edge_feat, edge_grad)
    grad_dest = jax.ops.segment_sum(grad_pre_edge, edge_dst, row_count)
    grad_extended = jax.ops.segment_sum(
        jnp.concatenate([numer_edge * gating, grad_pre_edge], 1),
        edge_src,
        row_count + halo_send.shape[0],
    )
    returned = return_sources(grad_extended[row_count:])
    grad_source = grad_extended[:row_count].at[halo_send].add(returned)
    proj_grad = jnp.concatenate(
        [grad_message, grad_source[:, :model_width], grad_dest, grad_source[:, model_width:]], 1
    ).astype(jnp.bfloat16)
    grad_w_proj = outer_product(hidden_low, proj_grad)
    grad_hidden = (
        grad_mixed
        + grad_two
        + times_transposed(proj_grad, w_proj)
        + times_transposed(qkv_grad, w_qkv)
    )
    weight_grads = (grad_w_proj, grad_w_edge, grad_w_qkv, grad_w_out, grad_w_up, grad_w_down)
    return (
        grad_hidden,
        weight_grads,
        jnp.stack([gain_one, gain_two, gain_three]),
        jnp.stack([shift_one, shift_two, shift_three]),
    )


def per_device(
    node_input,
    edge_feat,
    graph_ids,
    edge_src,
    edge_dst,
    halo_send,
    w_proj,
    w_edge,
    w_qkv,
    w_out,
    w_up,
    w_down,
    norm_gain,
    norm_shift,
    cotangent,
):
    group_graphs = lax.all_gather(graph_ids, "nodes", axis=0, tiled=True)
    node_total = node_input.shape[0] * lax.axis_size("nodes") * lax.axis_size("rep")
    layer_count = w_proj.shape[0]
    layer_params = [
        (
            w_proj[layer_index],
            w_edge[layer_index],
            w_qkv[layer_index],
            w_out[layer_index],
            w_up[layer_index],
            w_down[layer_index],
            norm_gain[layer_index],
            norm_shift[layer_index],
        )
        for layer_index in range(layer_count)
    ]
    hidden = node_input.astype(jnp.float32)
    saved_all = []
    for layer_index in range(layer_count):
        hidden, saved = layer_forward(
            hidden,
            layer_params[layer_index],
            edge_feat,
            edge_src,
            edge_dst,
            halo_send,
            graph_ids,
            group_graphs,
            node_total,
        )
        saved_all.append(saved)
    grad_hidden = cotangent.astype(jnp.float32)
    weight_parts = [None] * layer_count
    gain_parts = [None] * layer_count
    shift_parts = [None] * layer_count
    for layer_index in range(layer_count - 1, -1, -1):
        (
            grad_hidden,
            weight_parts[layer_index],
            gain_parts[layer_index],
            shift_parts[layer_index],
        ) = layer_backward(
            grad_hidden,
            layer_params[layer_index],
            saved_all[layer_index],
            edge_feat,
            edge_src,
            edge_dst,
            halo_send,
            graph_ids,
            group_graphs,
            node_total,
        )
    proj_local = jnp.stack([weight_parts[layer_index][0] for layer_index in range(layer_count)])
    edge_local = jnp.stack([weight_parts[layer_index][1] for layer_index in range(layer_count)])
    qkv_local = jnp.stack([weight_parts[layer_index][2] for layer_index in range(layer_count)])
    out_local = jnp.stack([weight_parts[layer_index][3] for layer_index in range(layer_count)])
    up_local = jnp.stack([weight_parts[layer_index][4] for layer_index in range(layer_count)])
    down_local = jnp.stack([weight_parts[layer_index][5] for layer_index in range(layer_count)])
    grad_proj, grad_edge, grad_qkv, grad_out, grad_up, grad_down = lax.psum(
        (proj_local, edge_local, qkv_local, out_local, up_local, down_local), ("nodes", "rep")
    )
    return (
        hidden,
        grad_hidden,
        grad_proj,
        grad_edge,
        grad_qkv,
        grad_out,
        grad_up,
        grad_down,
        jnp.stack(gain_parts),
        jnp.stack(shift_parts),
    )


def solution(mesh):
    in_specs = (
        P(("rep", "nodes"), None),
        P(("rep", "nodes"), None),
        P(("rep", "nodes")),
        P(("rep", "nodes")),
        P(("rep", "nodes")),
        P(("rep", "nodes")),
        P(),
        P(),
        P(),
        P(),
        P(),
        P(),
        P(),
        P(),
        P(("rep", "nodes"), None),
    )
    out_specs = (
        P(("rep", "nodes"), None),
        P(("rep", "nodes"), None),
        P(),
        P(),
        P(),
        P(),
        P(),
        P(),
        P(),
        P(),
    )
    N, M = mesh.shape["nodes"], mesh.shape["rep"]
    fused = N in (4, 8) and M % 2 == 0 and 512 % (16 * N * M) == 0
    return jax.shard_map(
        functools.partial(fused_device, N, M) if fused else per_device,
        mesh=mesh, in_specs=in_specs, out_specs=out_specs, check_vma=False,
    )
```

```python
import functools
import math

import jax
import jax.numpy as jnp
from jax import lax
from jax.experimental import pallas as pl
from jax.experimental.pallas import tpu as pltpu
from jax.sharding import PartitionSpec as P

HEADS = 8
HEAD_DIM = 32
NEG = -1e30
NORM_EPS = 1e-05
GATE_EPS = 1e-06
F32, BF16, I32 = jnp.float32, jnp.bfloat16, jnp.int32
MESH = pl.DeviceIdType.MESH
SYNCS = 12
STRIP = 32
GROUPS = (
    ("early", 1, 0, 2560, ("core", "y", "nodes")),
    ("conv", 1, 0, 2560, ("core", "x", "y", "z")),
    ("qkv", 1, 0, 1536, ("core", "y", "nodes")),
    ("early", 0, 0, 2560, ("core", "x", "y", "z")),
    ("conv", 0, 0, 2560, ("core", "y", "nodes")),
    ("qkv", 0, 0, 1536, ("rep", "nodes")),
)


def dot(left, right):
    return lax.dot_general(
        left, right, (((1,), (0,)), ((), ())), preferred_element_type=F32
    )


def dot_nt(left, right):
    return lax.dot_general(
        left, right, (((1,), (1,)), ((), ())), preferred_element_type=F32
    )


def dot_tn(left, right):
    return lax.dot_general(
        left, right, (((0,), (0,)), ((), ())), preferred_element_type=F32
    )


def split(value):
    high = value.astype(BF16)
    return high, (value - high.astype(F32)).astype(BF16)


def sigmoid(value):
    return jax.nn.sigmoid(value)


def silu_slope(value):
    logistic = sigmoid(value)
    return logistic * (1.0 + value * (1.0 - logistic))


def col_sum(value):
    return jnp.sum(value, axis=0, keepdims=True)


def pack(first, second):
    return jnp.concatenate([first[:, :128], first[:, 128:], second[:, :128], second[:, 128:]], 0)


def unpack(tile):
    return [jnp.concatenate([tile[i : i + 1], tile[i + 1 : i + 2]], 1) for i in (0, 2)]


def combine_moments(tiles, count):
    mean = jnp.mean(tiles[:, 0:2], 0)
    off = tiles[:, 0:2] - mean
    return jnp.concatenate([mean, jnp.sum(tiles[:, 2:4] + count * off * off, 0)], 0)


class Refs:
    pass


def axis_sizes(N, M):
    return dict(core=2, y=M // 2, x=2, z=N // 2, rep=M, nodes=N)


def scratch_list(N, M, L, R, E):
    NZ, NB, G = N // 2, N // 4, N * R
    D, FF, W, HH = 256, 512, 4 * R, HEADS // 2 * R
    dma = lambda *shape: pltpu.SemaphoreType.DMA(shape)
    vm = lambda dtype, *shape: pltpu.VMEM(shape, dtype)
    names = dict(
        gb=vm(BF16, L, N, R, D),
        xs=vm(BF16, L, N, R, D),
        meta=vm(I32, N, 8, 256),
        cot=vm(BF16, R, D),
        wp=vm(BF16, L, D, 4 * D),
        we=vm(BF16, L, D, D),
        wqkv=vm(BF16, L, D, 3 * D),
        wo=vm(BF16, L, D, D),
        wu=vm(BF16, L, D, FF),
        wd=vm(BF16, L, FF, D),
        st1=vm(F32, SYNCS, M * N, 4, 128),
        gain=vm(F32, L, 8, D),
        shift=vm(F32, L, 8, D),
        ggain=vm(F32, L, 8, D),
        gshift=vm(F32, L, 8, D),
        iv=vm(F32, L, 8, D),
        moff=vm(F32, N, 8, D),
        move=vm(F32, 8, D),
        le=vm(BF16, E, 1024),
        re=vm(BF16, 1024, D),
        TT=vm(BF16, R, 2 * E),
        ST=vm(BF16, 256, E),
        efT=vm(BF16, D, E),
        HP=vm(BF16, 32, R),
        HN=vm(BF16, 32, R),
        A=vm(BF16, R, 64),
        bias=vm(F32, R, G),
        xf=vm(F32, L + 1, R, D),
        xe=vm(BF16, L, 256, D),
        xeT=vm(BF16, D, 256),
        gate=vm(F32, L, E, D),
        bs=vm(BF16, L, E, D),
        num=vm(F32, L, R, D),
        den=vm(F32, L, R, D),
        z0=vm(F32, L, R, D),
        z1=vm(F32, L, R, D),
        z2=vm(F32, L, R, D),
        wkvT=vm(BF16, L, 2 * D, D),
        kvT=vm(BF16, L, 2 * D, G),
        odT=vm(F32, NB, D, R),
        ldT=vm(F32, NB, D, R),
        md=vm(F32, NB, R, D),
        rb=vm(F32, L, NB, R, D),
        pst=vm(BF16, L, HEADS * R, G),
        oraw=vm(F32, L, R, D),
        ob=vm(BF16, L, R, D),
        mb=vm(BF16, L, R, D),
        u=vm(F32, L, R, FF),
        g=vm(BF16, L, R, FF),
        dy=vm(F32, R, D),
        dmix=vm(F32, R, D),
        gy0=vm(F32, R, D),
        local=vm(F32, R, D),
        dxo=vm(F32, R, D),
        dob=vm(F32, R, D),
        dqT=vm(F32, D, R),
        qm=vm(BF16, L, 2, HH, 128),
        q=vm(BF16, L, R, D),
        qT=vm(BF16, D, R),
        dosT=vm(BF16, 128, R),
        dom=vm(BF16, HH, 256),
        sc=vm(F32, 2, max(2 * R, E), W),
        tp=vm(F32, HEADS // 2, R, 128),
        dss=vm(BF16, HH, W),
        dkv=vm(BF16, 2 * D, W),
        gkv=vm(F32, 2 * D, D),
        gg=vm(BF16, 2 * E, 2 * D),
        dn=vm(BF16, 512, 2 * D),
        dproj=vm(BF16, 256, 4 * D),
        dxs=vm(BF16, L, NZ, 2, R, D),
        rs1=vm(BF16, L, NZ, R, D),
        cs=vm(BF16, L, NZ, R, D),
        rs2=vm(BF16, L, NZ, R, D),
        ro=vm(BF16, L, 3, R, D),
        hs=vm(BF16, L, 2, 32, D),
        hr=vm(BF16, L, 2, 32, D),
    )
    names.update(
        gs_early=vm(BF16, L, 2560, 128),
        gs_conv=vm(BF16, L, 2560, 128),
        gs_qkv=vm(BF16, L, 1536, 128),
    )
    sizes = axis_sizes(N, M)
    for g, (_, _, _, rows, stages) in enumerate(GROUPS):
        names[f"go{g}"] = vm(BF16, rows, 128)
        left = rows
        for k, axis in enumerate(stages):
            left //= sizes[axis]
            names[f"ga{g}_{k}"] = vm(BF16, sizes[axis] - 1, left, 128)
            if k < len(stages) - 1:
                names[f"gh{g}_{k}"] = vm(BF16, left, 128)
    names.update(
        ar_s=dma(len(GROUPS), 8),
        ar_r=dma(len(GROUPS), 8),
        ar_l=dma(len(GROUPS)),
        load=dma(10),
        store=dma(2),
        meta_s=dma(1),
        meta_r=dma(1),
        st1_s=dma(SYNCS),
        st1_r=dma(SYNCS),
        agc_s=dma(L, NZ),
        agc_r=dma(L, NZ),
        agp_s=dma(L, NZ),
        agp_r=dma(L, NZ),
        rsp_s=dma(L, NZ),
        rsp_r=dma(L, NZ),
        ro_s=dma(L, 3),
        ro_r=dma(L, 3),
        rsc_s=dma(L, NZ),
        rsc_r=dma(L, NZ),
        hal_s=dma(L, 2),
        hal_r=dma(L, 2),
    )
    return names


IN_NAMES = (
    "x_in", "ids", "edge_src", "edge_dst", "halo", "ef_h", "wp_h", "we_h", "wqkv_h", "wo_h", "wu_h", "wd_h",
    "gain_in", "shift_in", "cot_h",
)
OUT_NAMES = ("out_act", "grad_in", *(f"gout{g}" for g in range(len(GROUPS))), "ggain_out", "gshift_out")


def kernel(N, M, L, names, *args):
    r_ = Refs()
    for name, ref in zip(IN_NAMES + OUT_NAMES + tuple(names), args, strict=True):
        setattr(r_, name, ref)
    R, D = r_.x_in.shape
    E = r_.ef_h.shape[0]
    NZ, NB, G, W = N // 2, N // 4, N * R, 4 * R
    HK = HEADS // 2
    total = float(N * M * R)
    scale = HEAD_DIM ** -0.5
    me = lax.axis_index("nodes")
    rep = lax.axis_index("rep")
    z = me // 2
    par = me % 2
    partner = 2 * z + (1 - par)
    prev = (me + N - 1) % N
    nxt = (me + 1) % N
    zh, zl = z // 2, z % 2
    z_to = lambda t: 2 * ((zh + t // 2) % NB) + (zl + t % 2) % 2
    z_from = lambda t: 2 * ((zh + NB - t // 2) % NB) + (zl + t % 2) % 2

    def remote(src, dst, s_sem, r_sem, **where):
        return pltpu.make_async_remote_copy(
            src_ref=src, dst_ref=dst, send_sem=s_sem, recv_sem=r_sem,
            device_id=where, device_id_type=MESH,
        )

    def send(src, dst, s_sem, r_sem, **where):
        remote(src, dst, s_sem, r_sem, **where).start()

    def send_rows(src, dst, rows, s_sem, r_sem, **where):
        pieces = next(p for p in range(1, rows) if rows % (16 * p) == 0 and rows // p <= 128)
        for at in range(0, rows, rows // pieces):
            cut = pl.ds(at, rows // pieces)
            send(src.at[cut], dst.at[cut], s_sem, r_sem, **where)

    def arrive(dst, r_sem):
        remote(dst, dst, r_sem, r_sem, nodes=partner).wait_recv()

    def sent(src, s_sem):
        remote(src, src, s_sem, s_sem, nodes=partner).wait_send()

    def when(condition, *acts):
        @pl.when(condition)
        def _():
            for act in acts:
                act()

    loads = [pltpu.make_async_copy(r_.ef_h, r_.le.at[:, D : 2 * D], r_.load.at[0])] + [
        pltpu.make_async_copy(getattr(r_, f"{name}_h"), getattr(r_, name), r_.load.at[1 + i])
        for i, name in enumerate(("we", "wqkv", "wp", "wo", "wu", "wd", "cot"))
    ]
    own_rows = pltpu.make_async_copy(r_.x_in, r_.gb.at[0, me], r_.load.at[8])
    own_rows.start()
    for load in loads:
        load.start()

    barrier = pltpu.get_barrier_semaphore()
    for dr in range(M):
        for d in range(N):
            if dr + d > 0:
                pl.semaphore_signal(barrier, inc=1, device_id={"rep": (rep + dr) % M, "nodes": (me + d) % N},
                                    device_id_type=MESH)
    pl.semaphore_wait(barrier, M * N - 1)

    def gather_start(l):
        mine = r_.gb.at[l, me]
        send_rows(mine, mine, R, r_.agp_s.at[l, 0], r_.agp_r.at[l, 0], nodes=partner)
        send_rows(mine, mine, R, r_.agc_s.at[l, 1], r_.agc_r.at[l, 1], nodes=2 * z_to(1) + par)
        send_rows(mine, mine, R, r_.agp_s.at[l, 1], r_.agp_r.at[l, 1], nodes=2 * z_to(1) + 1 - par)
        for t in range(2, NZ):
            send_rows(mine, mine, R, r_.agc_s.at[l, t], r_.agc_r.at[l, t], nodes=2 * z_to(t) + par)

    def gather_pass(l, t):
        piece = r_.gb.at[l, 2 * z_from(t) + par]
        arrive(piece, r_.agc_r.at[l, t])
        send_rows(piece, piece, R, r_.agp_s.at[l, t], r_.agp_r.at[l, t], nodes=partner)

    def gather_take(l, t):
        arrive(r_.gb.at[l, 2 * z_from(t) + 1 - par], r_.agp_r.at[l, t])

    def sync_start(k, first, second):
        mine = rep * N + me
        r_.st1[k, mine] = pack(first, second)
        for dr in range(M):
            for d in range(N):
                if dr + d > 0:
                    send(r_.st1.at[k, mine], r_.st1.at[k, mine], r_.st1_s.at[k], r_.st1_r.at[k],
                         rep=(rep + dr) % M, nodes=(me + d) % N)

    def sync_wait(k):
        arrive(r_.st1.at[k, 0 : M * N - 1], r_.st1_r.at[k])

    def sync_moments(k):
        sync_wait(k)
        return unpack(combine_moments(r_.st1[k], float(R)))

    def sync_sums(k):
        sync_wait(k)
        return unpack(jnp.sum(r_.st1[k], 0))

    sizes = axis_sizes(N, M)
    core, row = rep % 2, rep // 2
    places = dict(
        core=(core, lambda t: dict(rep=2 * row + t)),
        y=(row, lambda t: dict(rep=2 * t + core)),
        x=(par, lambda t: dict(nodes=2 * z + t)),
        z=(z, lambda t: dict(nodes=2 * t + par)),
        rep=(rep, lambda t: dict(rep=t)),
        nodes=(me, lambda t: dict(nodes=t)),
    )

    def reduce_step(g, step):
        name, layer, first, rows, stages = GROUPS[g]
        K = len(stages)
        gs, out = getattr(r_, f"gs_{name}").at[layer, first : first + rows], getattr(r_, f"go{g}")
        count, offset = [rows], [0]
        for axis in stages:
            count.append(count[-1] // sizes[axis])
            offset.append(offset[-1] + places[axis][0] * count[-1])
        take = lambda start, size: pl.ds(pl.multiple_of(start, 16), size)
        if 1 <= step <= K:
            k = step - 1
            got = getattr(r_, f"ga{g}_{k}")
            arrive(got, r_.ar_r.at[g, k])
            held = gs if k == 0 else getattr(r_, f"gh{g}_{k - 1}")
            index = places[stages[k]][0]
            acc = held[take(index * count[k + 1], count[k + 1])].astype(F32)
            for slot in range(sizes[stages[k]] - 1):
                acc = acc + got[slot].astype(F32)
            if step < K:
                getattr(r_, f"gh{g}_{k}")[...] = acc.astype(BF16)
            else:
                out[take(offset[K], count[K])] = acc.astype(BF16)
        elif step > K:
            k = 2 * K - step
            arrive(out.at[0 : (sizes[stages[k]] - 1) * count[k + 1]], r_.ar_r.at[g, step - 1])
        if step < K:
            held = gs if step == 0 else getattr(r_, f"gh{g}_{step - 1}")
            index, device = places[stages[step]]
            size = sizes[stages[step]]
            for d in range(1, size):
                to = (index + d) % size
                send_rows(held.at[take(to * count[step + 1], count[step + 1])], getattr(r_, f"ga{g}_{step}").at[d - 1],
                     count[step + 1], r_.ar_s.at[g, step], r_.ar_r.at[g, step], **device(to))
        elif step < 2 * K:
            k = 2 * K - 1 - step
            index, device = places[stages[k]]
            size = sizes[stages[k]]
            here = out.at[take(offset[k + 1], count[k + 1])]
            for d in range(1, size):
                send_rows(here, here, count[k + 1], r_.ar_s.at[g, step], r_.ar_r.at[g, step],
                          **device((index + d) % size))
        else:
            pltpu.make_async_copy(out, getattr(r_, f"gout{g}"), r_.ar_l.at[g]).start()

    def reduce_drain(g):
        _, _, _, rows, stages = GROUPS[g]
        K, left = len(stages), rows
        out = getattr(r_, f"go{g}")
        for k, axis in enumerate(stages):
            left //= sizes[axis]
            for step in (k, 2 * K - 1 - k):
                sent(out.at[0 : (sizes[axis] - 1) * left], r_.ar_s.at[g, step])
        pltpu.make_async_copy(out, getattr(r_, f"gout{g}"), r_.ar_l.at[g]).wait()

    def put(buf, l, at, value):
        rows = value.shape[0]
        for c in range(value.shape[1] // 128):
            buf[l, at : at + rows] = value[:, 128 * c : 128 * (c + 1)].astype(BF16)
            at += rows
        return at

    lane_head = lax.broadcasted_iota(I32, (R, 128), 1) // HEAD_DIM

    def by_head(parts):
        out = parts[0]
        for k in range(1, HK):
            out = jnp.where(lane_head == k, parts[k], out)
        return out

    r_.meta[me] = jnp.full((8, 256), -1, I32)
    r_.meta[me, 0:1, 0:R] = r_.ids[...].reshape(1, R)
    r_.meta[me, 1:2, 0:48] = r_.halo[...].reshape(1, 48)
    for d in range(1, N):
        send(r_.meta.at[me], r_.meta.at[me], r_.meta_s.at[0], r_.meta_r.at[0], nodes=(me + d) % N)
    own_rows.wait()
    gather_start(0)

    src_row = r_.edge_src[...].reshape(1, E)
    src_row = jnp.where(src_row < R + 24, src_row, src_row + 8)
    dst_row = r_.edge_dst[...].reshape(1, E)
    src_col = jnp.broadcast_to(src_row, (128, E)).T[:, 0:1]
    dst_col = jnp.broadcast_to(dst_row, (128, E)).T[:, 0:1]
    as_mask = lambda cond: cond.astype(F32).astype(BF16)
    r_.le[:, 0:256] = as_mask(src_col == lax.broadcasted_iota(I32, (E, 256), 1))
    target = as_mask(dst_col == lax.broadcasted_iota(I32, (E, 256), 1))
    r_.le[:, 512:768] = target
    r_.le[:, 768:1024] = target
    target = as_mask(dst_row == lax.broadcasted_iota(I32, (R, E), 0))
    r_.TT[:, 0:E] = target
    r_.TT[:, E:] = target
    r_.ST[...] = as_mask(src_row == lax.broadcasted_iota(I32, (256, E), 0))
    r_.dn[R:256] = jnp.zeros((256 - R, 2 * D), BF16)
    r_.dn[256 + R : 512] = jnp.zeros((256 - R, 2 * D), BF16)
    r_.dproj[R:256, 0:D] = jnp.zeros((256 - R, D), BF16)
    r_.dproj[R:256, 2 * D : 3 * D] = jnp.zeros((256 - R, D), BF16)
    loads[0].wait()
    r_.efT[...] = r_.le[:, D : 2 * D].T
    for l in range(L):
        for k in range(3):
            r_.gain[l, k : k + 1] = r_.gain_in[k, l : l + 1]
            r_.shift[l, k : k + 1] = r_.shift_in[k, l : l + 1]
    r_.xf[0] = r_.gb[0, me].astype(F32)
    r_.moff[...] = jnp.zeros((N, 8, D), F32)
    r_.move[0:1] = jnp.ones((1, D), F32)
    r_.move[1:2] = jnp.zeros((1, D), F32)
    for load in loads[1:]:
        load.wait()
    for l in range(L):
        r_.wkvT[l] = r_.wqkv[l, :, D:].T

    arrive(r_.meta.at[0 : N - 1], r_.meta_r.at[0])
    id_col = jnp.broadcast_to(r_.meta[me][0:1, 0:R], (128, R)).T[:, 0:1]
    id_row = jnp.concatenate([r_.meta[j][0:1, 0:R] for j in range(N)], 1)
    r_.bias[...] = jnp.where(id_col == id_row, 0.0, NEG)

    def halo_onehot(device, start):
        col = jnp.broadcast_to(r_.meta[device][1:2, 0:128], (128, 128)).T[start : start + 24, 0:1]
        hot = (col == lax.broadcasted_iota(I32, (24, R), 1)).astype(F32)
        return jnp.concatenate([hot, jnp.zeros((8, R), F32)], 0).astype(BF16)

    r_.HP[...] = halo_onehot(prev, 24)
    r_.HN[...] = halo_onehot(nxt, 0)
    r_.A[...] = as_mask(r_.meta[me][1:2, 0:64] == lax.broadcasted_iota(I32, (R, 64), 0))

    factor_exp = scale * math.log2(math.e)

    def prepare_queries(l):
        q = dot(r_.xs[l, me], r_.wqkv[l, :, :D]).astype(BF16)
        r_.q[l] = q
        q = q.astype(F32)
        for hf in range(2):
            for k in range(HK):
                part = jnp.where(lane_head == k, q[:, 128 * hf : 128 * (hf + 1)], 0.0)
                r_.qm[l, hf, k * R : (k + 1) * R] = part.astype(BF16)

    def head_dims(hf, k, base=0):
        return pl.ds(pl.multiple_of(base + hf * 128 + k * HEAD_DIM, HEAD_DIM), HEAD_DIM)

    def head_rows(hf, k, count=1):
        return pl.ds(pl.multiple_of((hf * HK + k) * R, 64), count * R)

    def lane_half(hf):
        return pl.ds(pl.multiple_of(hf * 128, 128), 128)

    def attention_block(l, i, middle):
        half = (zh + NB - i) % NB
        rows = pl.ds(pl.multiple_of(half * W, 128), W)
        x = r_.xs[l, pl.ds(4 * half, 4)].reshape(W, D)
        r_.kvT[l, :, rows] = dot_nt(r_.wkvT[l], x).astype(BF16)

        def heads(hf, carry):
            lanes = lane_half(hf)
            ones = jnp.ones((HEAD_DIM, W), BF16)
            for c in range(HK // 2):
                r_.sc[c % 2, 0 : 2 * R] = dot(r_.qm[l, hf, 2 * c * R : 2 * (c + 1) * R], r_.kvT[l, lanes, rows])
                for k in range(2):
                    for at in range(0, R, STRIP):
                        s = r_.sc[c % 2, k * R + at : k * R + at + STRIP] + r_.bias[at : at + STRIP, rows]
                        top = jnp.max(s, 1, keepdims=True)
                        e = jnp.exp2((s - top) * factor_exp)
                        r_.tp[2 * c + k, at : at + STRIP] = jnp.broadcast_to(top, (STRIP, 128))
                        first = pl.multiple_of((hf * HK + 2 * c + k) * R + at, STRIP)
                        r_.pst[l, pl.ds(first, STRIP), rows] = e.astype(BF16)
                for k in range(2):
                    h = 2 * c + k
                    left = jnp.concatenate([r_.kvT[l, head_dims(hf, h, D), rows], ones], 0)
                    o = dot_nt(left, r_.pst[l, head_rows(hf, h), rows])
                    r_.odT[i, head_dims(hf, h)] = o[0:HEAD_DIM]
                    r_.ldT[i, head_dims(hf, h)] = o[HEAD_DIM:]
            r_.md[i, :, lanes] = by_head([r_.tp[k] for k in range(HK)])
            middle(i, hf)
            return carry

        lax.fori_loop(0, 2, heads, 0)

    def attention_end(l):
        tops = [r_.md[i].T for i in range(NB)]
        top = tops[0]
        for i in range(1, NB):
            top = jnp.maximum(top, tops[i])
        factors = [jnp.exp2((tops[i] - top) * factor_exp) for i in range(NB)]
        inv = 1.0 / sum(factors[i] * r_.ldT[i] for i in range(NB))
        o = jnp.zeros((D, R), F32)
        for i in range(NB):
            r_.rb[l, i] = (factors[i] * inv).T
            o = o + factors[i] * inv * r_.odT[i]
        o = o.T
        r_.oraw[l] = o
        ob = o.astype(BF16)
        r_.ob[l] = ob
        t1 = r_.xf[l] + dot(ob, r_.wo[l])
        r_.z1[l] = t1
        mean1 = col_sum(t1) / R
        return mean1, col_sum((t1 - mean1) * (t1 - mean1))

    def convolution(l):
        xs = r_.xs
        xb = xs[l, me]
        r_.xe[l, 0:R] = xb
        r_.xe[l, R : R + 32] = dot(r_.HP[...], xs[l, prev]).astype(BF16)
        r_.xe[l, R + 32 : R + 64] = dot(r_.HN[...], xs[l, nxt]).astype(BF16)
        xe = r_.xe[l]
        made = dot(xe, r_.wp[l])
        pd_high, pd_low = split(made[:, 2 * D : 3 * D])
        r_.re[0:256] = made[:, 3 * D :].astype(BF16)
        r_.re[256:512] = r_.we[l]
        r_.re[512:768] = pd_high
        r_.re[768:1024] = pd_low
        r_.gate[l] = dot(r_.le[...], r_.re[...])
        r_.bs[l] = dot(r_.le[:, 0:256], made[:, D : 2 * D].astype(BF16)).astype(BF16)
        for at in range(0, E, 64):
            here = slice(at, at + 64)
            gate = sigmoid(r_.gate[l, here])
            r_.gate[l, here] = gate
            high, low = split(jnp.concatenate([gate * r_.bs[l, here].astype(F32), gate], 1))
            r_.gg[here] = high
            r_.gg[E + at : E + at + 64] = low
        num_den = dot(r_.TT[...], r_.gg[...])
        pa, num, den = made[0:R, 0:D], num_den[:, 0:D], num_den[:, D:]
        r_.num[l] = num
        r_.den[l] = den
        msg = pa + num / (den + GATE_EPS)
        r_.z0[l] = msg
        mean0 = col_sum(msg) / R
        sync_start(3 * l, mean0, col_sum((msg - mean0) * (msg - mean0)))

    def forward(l, carry):
        def ready(js):
            for j in js:
                moved = (r_.gb[l, j].astype(F32) + r_.moff[j, 0:1]) * r_.move[0:1] + r_.move[1:2]
                r_.xs[l, j] = moved.astype(BF16)

        r_.xs[l, me] = r_.xf[l].astype(BF16)
        prepare_queries(l)
        arrive(r_.gb.at[l, 2 * z_from(1) + par], r_.agc_r.at[l, 1])
        gather_take(l, 0)
        gather_take(l, 1)
        ready([partner, 2 * z_from(1) + par, 2 * z_from(1) + 1 - par])

        def middle(i, hf):
            when((i == 0) & (hf == 0), *[functools.partial(gather_pass, l, t) for t in range(2, NZ)])

        def block(i, carry):
            attention_block(l, i, middle)

            @pl.when(i == 0)
            def _():
                for t in range(2, NZ):
                    gather_take(l, t)
                ready([2 * z_from(t) + p for t in range(2, NZ) for p in range(2)])
                convolution(l)

            return carry

        lax.fori_loop(0, NB, block, 0)
        mean1, sq1 = attention_end(l)
        sync_start(3 * l + 1, mean1, sq1)
        mean0, sq0 = sync_moments(3 * l)
        inv0 = lax.rsqrt(sq0 / total + NORM_EPS)
        r_.iv[l, 0:1] = inv0
        z0 = (r_.z0[l] - mean0) * inv0
        r_.z0[l] = z0
        n0 = z0 * r_.gain[l, 0:1] + r_.shift[l, 0:1]
        r_.local[...] = r_.xf[l] + n0 * sigmoid(n0)
        mean1, sq1 = sync_moments(3 * l + 1)
        inv1 = lax.rsqrt(sq1 / total + NORM_EPS)
        r_.iv[l, 1:2] = inv1
        z1 = (r_.z1[l] - mean1) * inv1
        r_.z1[l] = z1
        mix = r_.local[...] + z1 * r_.gain[l, 1:2] + r_.shift[l, 1:2]
        mb = mix.astype(BF16)
        r_.mb[l] = mb
        u = dot(mb, r_.wu[l])
        r_.u[l] = u
        g = (u * sigmoid(u)).astype(BF16)
        r_.g[l] = g
        y = mix + dot(g, r_.wd[l])
        r_.z2[l] = y
        mean = col_sum(y) / R
        cent = y - mean
        k = 3 * l + 2
        sync_start(k, mean, col_sum(cent * cent))

        @pl.when(l < L - 1)
        def _():
            r_.gb[l + 1, me] = cent.astype(BF16)
            gather_start(l + 1)

        @pl.when(l == L - 1)
        def _():
            dy = r_.cot[...].astype(F32)
            sync_start(3 * L, col_sum(dy), col_sum(dy * cent))

        tot_mean, tot_sq = sync_moments(k)
        inv2 = lax.rsqrt(tot_sq / total + NORM_EPS)
        r_.iv[l, 2:3] = inv2
        z2 = (r_.z2[l] - tot_mean) * inv2
        r_.z2[l] = z2
        gain, shift = r_.gain[l, 2:3], r_.shift[l, 2:3]
        r_.xf[l + 1] = z2 * gain + shift

        @pl.when(l == L - 1)
        def _():
            sync_wait(3 * L)
            sums, means = r_.st1[3 * L], r_.st1[k][:, 0:2]
            mean = jnp.mean(means, 0)
            dy_sum = jnp.sum(sums[:, 0:2], 0)
            dy_cent = jnp.sum(sums[:, 2:4] + (means - mean) * sums[:, 0:2], 0)
            dy_sum, dy_cent = unpack(jnp.concatenate([dy_sum, dy_cent], 0))
            r_.gshift[l, 2:3] = dy_sum
            r_.ggain[l, 2:3] = dy_cent * inv2

        for j in range(N):
            tile = r_.st1[k, rep * N + j]
            r_.moff[j, 0:1] = jnp.concatenate([tile[0:1], tile[1:2]], 1) - tot_mean
        r_.move[0:1] = inv2 * gain
        r_.move[1:2] = shift
        return carry

    lax.fori_loop(0, L, forward, 0)
    act_copy = pltpu.make_async_copy(r_.xf.at[L], r_.out_act, r_.store.at[0])
    act_copy.start()

    def back_feed_forward(l, k):
        s2, g2 = r_.gshift[l, 2:3], r_.ggain[l, 2:3]
        d3 = r_.gain[l, 2:3] * r_.iv[l, 2:3] * (r_.dy[...] - s2 / total - r_.z2[l] * (g2 / total))
        db = d3.astype(BF16)
        dub = (dot_nt(db, r_.wd[l]) * silu_slope(r_.u[l])).astype(BF16)
        dmix = d3 + dot_nt(dub, r_.wu[l])
        r_.dmix[...] = dmix
        n0 = r_.z0[l] * r_.gain[l, 0:1] + r_.shift[l, 0:1]
        gy0 = dmix * silu_slope(n0)
        sync_start(k, col_sum(dmix), col_sum(dmix * r_.z1[l]))
        sync_start(k + 1, col_sum(gy0), col_sum(gy0 * r_.z0[l]))
        r_.gy0[...] = gy0
        at = put(r_.gs_early, l, 512, dot_tn(r_.mb[l], dub))
        put(r_.gs_early, l, at, dot_tn(r_.g[l], db))
        r_.xeT[...] = r_.xe[l].T
        r_.qT[...] = r_.q[l].T

    def back_norms(l, k):
        s1, g1 = sync_sums(k)
        r_.gshift[l, 1:2] = s1
        r_.ggain[l, 1:2] = g1
        dmix = r_.dmix[...]
        d2 = r_.gain[l, 1:2] * r_.iv[l, 1:2] * (dmix - s1 / total - r_.z1[l] * (g1 / total))
        dab = d2.astype(BF16)
        r_.dxo[...] = dmix + d2
        r_.dob[...] = dot_nt(dab, r_.wo[l]).astype(BF16).astype(F32)
        put(r_.gs_early, l, 0, dot_tn(r_.ob[l], dab))
        r_.gkv[...] = jnp.zeros((2 * D, D), F32)
        r_.dqT[...] = jnp.zeros((D, R), F32)

    def back_attention_block(l, i, between):
        t1 = (i + 1) % NB
        half = (zh + t1) % NB
        rows = pl.ds(pl.multiple_of(half * W, 128), W)

        def heads(hf, carry):
            lanes = lane_half(hf)
            dos = r_.dob[:, lanes] * r_.rb[l, (NB - t1) % NB, :, lanes]
            prod = dos * r_.oraw[l, :, lanes]
            for k in range(HK):
                r_.dom[k * R : (k + 1) * R, 0:128] = jnp.where(lane_head == k, dos, 0.0).astype(BF16)
                r_.dom[k * R : (k + 1) * R, 128:256] = jnp.where(lane_head == k, -prod, 0.0).astype(BF16)
            r_.dosT[...] = dos.T.astype(BF16)
            values = pl.ds(pl.multiple_of(D + hf * 128, 128), 128)
            right = jnp.concatenate([r_.kvT[l, values, rows], jnp.ones((128, W), BF16)], 0)
            for c in range(HK // 2):
                both = slice(2 * c * R, 2 * (c + 1) * R)
                r_.sc[c % 2, 0 : 2 * R] = dot(r_.dom[both], right)
                for k in range(2):
                    for at in range(0, R, STRIP):
                        first = pl.multiple_of((hf * HK + 2 * c + k) * R + at, STRIP)
                        e = r_.pst[l, pl.ds(first, STRIP), rows].astype(F32)
                        ds = e * r_.sc[c % 2, k * R + at : k * R + at + STRIP]
                        r_.dss[(2 * c + k) * R + at : (2 * c + k) * R + at + STRIP] = ds.astype(BF16)
                for k in range(2):
                    h = 2 * c + k
                    mine, dims = slice(h * R, (h + 1) * R), head_dims(hf, h)
                    r_.dqT[dims] += dot_nt(r_.kvT[l, dims, rows], r_.dss[mine])
                    r_.dkv[dims] = (dot(r_.qT[dims], r_.dss[mine]) * scale).astype(BF16)
                    dv = dot(r_.dosT[h * HEAD_DIM : (h + 1) * HEAD_DIM], r_.pst[l, head_rows(hf, h), rows])
                    r_.dkv[head_dims(hf, h, D)] = dv.astype(BF16)
            between(i, hf)
            return carry

        lax.fori_loop(0, 2, heads, 0)
        dx = dot(r_.wqkv[l, :, D:], r_.dkv[...]).T
        r_.dxs[l, pl.ds(2 * half, 2)] = dx.astype(BF16).reshape(2, 2, R, D)

        @pl.when(i < NB - 1)
        def _():
            for low in range(2):
                zb = 2 * half + low
                send_rows(r_.dxs.at[l, zb, 1 - par], r_.rs1.at[l, zb], R,
                     r_.rsp_s.at[l, 2 * i + low], r_.rsp_r.at[l, 2 * i + low], nodes=partner)

        @pl.when(i == NB - 1)
        def _():
            near = z_to(1)
            send_rows(r_.dxs.at[l, z, 1 - par], r_.ro.at[l, 0], R, r_.ro_s.at[l, 0], r_.ro_r.at[l, 0], nodes=partner)
            send_rows(r_.dxs.at[l, near, par], r_.ro.at[l, 1], R, r_.ro_s.at[l, 1], r_.ro_r.at[l, 1], nodes=2 * near + par)
            send_rows(r_.dxs.at[l, near, 1 - par], r_.ro.at[l, 2], R, r_.ro_s.at[l, 2], r_.ro_r.at[l, 2],
                 nodes=2 * near + 1 - par)

        r_.gkv[...] += dot(r_.dkv[...], r_.xs[l, pl.ds(4 * half, 4)].reshape(W, D))

    def pass_on(l, i, t):
        zb = z_to(t)
        arrive(r_.rs1.at[l, zb], r_.rsp_r.at[l, 2 * i + zb % 2])
        both = r_.dxs[l, zb, par].astype(F32) + r_.rs1[l, zb].astype(F32)
        r_.cs[l, zb] = both.astype(BF16)
        send_rows(r_.cs.at[l, zb], r_.rs2.at[l, z], R, r_.rsc_s.at[l, t], r_.rsc_r.at[l, t], nodes=2 * zb + par)

    def back_convolution(l, k):
        s0, g0 = sync_sums(k + 1)
        r_.gshift[l, 0:1] = s0
        r_.ggain[l, 0:1] = g0
        inv_den = 1.0 / (r_.den[l] + GATE_EPS)
        dm = r_.gain[l, 0:1] * r_.iv[l, 0:1] * (r_.gy0[...] - s0 / total - r_.z0[l] * (g0 / total))
        dnum = dm * inv_den
        dden = -dnum * r_.num[l] * inv_den
        high, low = split(jnp.concatenate([dnum, dden], 1))
        r_.dn[0:R] = high
        r_.dn[256 : 256 + R] = low
        r_.sc[0, 0:E, 0 : 2 * D] = dot(r_.le[:, 512:1024], r_.dn[...])
        for at in range(0, E, 64):
            here = slice(at, at + 64)
            gate, dnum_e = r_.gate[l, here], r_.sc[0, here, 0:D]
            dgp = (dnum_e * r_.bs[l, here].astype(F32) + r_.sc[0, here, D : 2 * D]) * gate * (1.0 - gate)
            r_.gg[here, 0:D] = (dnum_e * gate).astype(BF16)
            r_.gg[here, D:] = dgp.astype(BF16)
        ext = dot(r_.ST[...], r_.gg[0:E]).astype(BF16)
        r_.dproj[0:R, 0:D] = dm.astype(BF16)
        r_.dproj[:, D : 2 * D] = ext[:, 0:D]
        r_.dproj[0:R, 2 * D : 3 * D] = dot(r_.TT[:, 0:E], r_.gg[0:E, D:]).astype(BF16)
        r_.dproj[:, 3 * D :] = ext[:, D:]
        dxe = dot_nt(r_.dproj[...], r_.wp[l])
        r_.hs[l, 0] = dxe[R : R + 32].astype(BF16)
        r_.hs[l, 1] = dxe[R + 32 : R + 64].astype(BF16)
        send(r_.hs.at[l, 0], r_.hr.at[l, 1], r_.hal_s.at[l, 0], r_.hal_r.at[l, 0], nodes=prev)
        send(r_.hs.at[l, 1], r_.hr.at[l, 0], r_.hal_s.at[l, 1], r_.hal_r.at[l, 1], nodes=nxt)
        r_.dxo[...] += dxe[0:R]

    def conv_weight_grads(l):
        at = put(r_.gs_conv, l, 0, dot(r_.xeT[...], r_.dproj[...]))
        put(r_.gs_conv, l, at, dot(r_.efT[...], r_.gg[0:E, D:]))

    def back_input(l):
        dx = r_.dxo[...]
        dx = dx + r_.dxs[l, z, par].astype(F32)
        for slot in range(3):
            arrive(r_.ro.at[l, slot], r_.ro_r.at[l, slot])
            dx = dx + r_.ro[l, slot].astype(F32)
        for t in range(2, NZ):
            c = z_from(t)
            arrive(r_.rs2.at[l, c], r_.rsc_r.at[l, t])
            dx = dx + r_.rs2[l, c].astype(F32)
        arrive(r_.hr.at[l, 0], r_.hal_r.at[l, 1])
        arrive(r_.hr.at[l, 1], r_.hal_r.at[l, 0])
        back = jnp.concatenate(
            [r_.hr[l, 0].astype(F32)[0:24], r_.hr[l, 1].astype(F32)[0:24], jnp.zeros((16, D), F32)], 0
        )
        return dx + dot(r_.A[...], back.astype(BF16))

    r_.dy[...] = r_.cot[...].astype(F32)

    E1, C1, Q1, E0, C0, Q0 = range(len(GROUPS))

    def steps(*pairs):
        return [functools.partial(reduce_step, g, k) for g, k in pairs]

    r_.dy[...] = r_.cot[...].astype(F32)

    def backward(b, carry):
        l = L - 1 - b
        first, last = b == 0, b == L - 1
        k = 3 * L + 1 + 2 * b
        conv = functools.partial(back_convolution, l, k)
        conv_grads = functools.partial(conv_weight_grads, l)
        back_feed_forward(l, k)
        back_norms(l, k)
        when(first, *steps((E1, 0)))
        when(last, *steps((E1, 3), (C1, 1), (Q1, 1), (E0, 0)), conv, conv_grads,
             *steps((C1, 2), (Q1, 2), (E1, 4), (E0, 1), (C0, 0)))

        def between(i, hf):
            when(first & (i == 0) & (hf == 0), *steps((E1, 1)))
            when(first & (i == 1) & (hf == 0), *steps((E1, 2)))
            when(last & (i == 0) & (hf == 0), *steps((C0, 1)))
            when(last & (i == 0) & (hf == 1), *steps((E0, 2), (C1, 3), (Q1, 3), (E1, 5)))
            when(last & (i == 1) & (hf == 0), *steps((E0, 3), (C0, 2), (C1, 4), (Q1, 4), (E1, 6)))
            when(last & (i == 1) & (hf == 1), *steps((E0, 4), (C1, 5), (Q1, 5)))
            for t in range(2, NZ):
                when((i == 1) & (hf == 0), functools.partial(pass_on, l, 0, t))

        def block(i, carry):
            back_attention_block(l, i, between)
            return carry

        lax.fori_loop(0, NB, block, 0)
        when(first, conv)
        dqb = (r_.dqT[...].T * scale).astype(BF16)
        r_.dxo[...] += dot_nt(dqb, r_.wqkv[l, :, 0:D])
        when(first, conv_grads, *steps((C1, 0)))
        at = put(r_.gs_qkv, l, 0, dot(r_.xeT[:, 0:R], dqb))
        put(r_.gs_qkv, l, at, r_.gkv[...].T)

        @pl.when(first)
        def _():
            dx = back_input(l)
            r_.dy[...] = dx
            below = L - 2
            sync_start(SYNCS - 1, col_sum(dx), col_sum(dx * r_.z2[below]))
            reduce_step(Q1, 0)
            s2, g2 = sync_sums(SYNCS - 1)
            r_.gshift[below, 2:3] = s2
            r_.ggain[below, 2:3] = g2

        return carry

    lax.fori_loop(0, L, backward, 0)
    for step in steps((Q0, 0), (C0, 3), (E0, 5), (C1, 6), (Q1, 6), (Q0, 1)):
        step()
    r_.dy[...] = back_input(0)
    in_copy = pltpu.make_async_copy(r_.dy, r_.grad_in, r_.store.at[1])
    in_copy.start()
    for step in steps(
        (C0, 4), (E0, 6), (C1, 7), (Q0, 2),
        (C0, 5), (E0, 7), (C1, 8), (Q0, 3),
        (C0, 6), (E0, 8), (Q0, 4),
    ):
        step()
    for l in range(L):
        for k in range(3):
            r_.ggain_out[k, l : l + 1] = r_.ggain[l, k : k + 1]
            r_.gshift_out[k, l : l + 1] = r_.gshift[l, k : k + 1]
    for g in range(len(GROUPS)):
        reduce_drain(g)
    sent(r_.meta.at[0 : N - 1], r_.meta_s.at[0])
    for k in range(SYNCS):
        sent(r_.st1.at[k, 0 : M * N - 1], r_.st1_s.at[k])
    for l in range(L):
        for t in range(NZ):
            sent(r_.gb.at[l, 0], r_.agp_s.at[l, t])
            if t > 0:
                sent(r_.gb.at[l, 0], r_.agc_s.at[l, t])
            if t > 1:
                sent(r_.rs1.at[l, 0], r_.rsc_s.at[l, t])
        for slot in range(2 * (NB - 1)):
            sent(r_.rs1.at[l, 0], r_.rsp_s.at[l, slot])
        for slot in range(3):
            sent(r_.ro.at[l, 0], r_.ro_s.at[l, slot])
        for side in range(2):
            sent(r_.hs.at[l, 0], r_.hal_s.at[l, side])
    act_copy.wait()
    in_copy.wait()


def finish_kernel(act_h, gin_h, *refs):
    n = len(GROUPS)
    held, (ggain_h, gshift_h), refs = refs[:n], refs[n : n + 2], refs[n + 2 :]
    act_o, gin_o, proj_o, edge_o, qkv_o, out_o, up_o, down_o, ggain_o, gshift_o = refs[:10]
    summed, refs = refs[10 : 10 + n], refs[10 + n :]
    act, gin, proj, edge, qkv, out, up, down, in_sem, out_sem = refs
    loads = [
        pltpu.make_async_copy(src, dst, in_sem.at[i])
        for i, (src, dst) in enumerate(zip(held + (act_h, gin_h), summed + (act, gin), strict=True))
    ]
    for load in loads:
        load.start()
    ggain_o[...] = ggain_h[...]
    gshift_o[...] = gshift_h[...]
    stores = []

    def store(src, dst):
        copy = pltpu.make_async_copy(src, dst, out_sem.at[len(stores)])
        copy.start()
        stores.append(copy)

    def widen(dst, l, g, at, first=0, last=None):
        rows = dst.shape[1]
        for c in range(first, dst.shape[2] // 128 if last is None else last):
            dst[l, :, 128 * c : 128 * (c + 1)] = summed[g][at : at + rows].astype(F32)
            at += rows
        return at

    for g, (name, l, first, rows, _) in enumerate(GROUPS):
        loads[g].wait()
        if name == "early":
            at = widen(out, l, g, 0)
            store(out.at[l], out_o.at[l])
            at = widen(up, l, g, at)
            store(up.at[l], up_o.at[l])
            widen(down, l, g, at)
            store(down.at[l], down_o.at[l])
        elif name == "conv":
            at = widen(proj, l, g, 0)
            store(proj.at[l], proj_o.at[l])
            widen(edge, l, g, at)
            store(edge.at[l], edge_o.at[l])
        else:
            widen(qkv, l, g, 0, first // 256, (first + rows) // 256)
            if first + rows == 1536:
                store(qkv.at[l], qkv_o.at[l])
    for i, (src, dst) in enumerate(((act, act_o), (gin, gin_o))):
        loads[n + i].wait()
        store(src, dst)
    for copy in stores:
        copy.wait()


def fused_device(
    N, M, node_input, edge_feat, graph_ids, edge_src, edge_dst, halo_send, w_proj, w_edge, w_qkv,
    w_out, w_up, w_down, norm_gain, norm_shift, cotangent,
):
    R, D = node_input.shape
    E = edge_feat.shape[0]
    L = w_proj.shape[0]
    names = scratch_list(N, M, L, R, E)
    vmem = pl.BlockSpec(memory_space=pltpu.VMEM)
    hbm = pl.BlockSpec(memory_space=pltpu.HBM)
    shape = jax.ShapeDtypeStruct
    rows = shape((R, D), F32)
    norm = shape((3, L, D), F32)
    groups = [shape((rows_g, 128), BF16) for _, _, _, rows_g, _ in GROUPS]
    outs = pl.pallas_call(
        functools.partial(kernel, N, M, L, tuple(names)),
        out_shape=[rows, rows, *groups, norm, norm],
        in_specs=[hbm] + [vmem] * 4 + [hbm] * 7 + [vmem] * 2 + [hbm],
        out_specs=[hbm] * (2 + len(GROUPS)) + [vmem] * 2,
        scratch_shapes=list(names.values()),
        compiler_params=pltpu.CompilerParams(
            collective_id=0, has_side_effects=True, vmem_limit_bytes=60 << 20
        ),
        name="layers",
    )(node_input, graph_ids, edge_src, edge_dst, halo_send, edge_feat, w_proj, w_edge, w_qkv, w_out, w_up,
      w_down, norm_gain.transpose(1, 0, 2), norm_shift.transpose(1, 0, 2), cotangent)
    weights = [shape(w.shape, F32) for w in (w_proj, w_edge, w_qkv, w_out, w_up, w_down)]
    results = pl.pallas_call(
        finish_kernel,
        out_shape=[rows, rows, *weights, norm, norm],
        in_specs=[hbm] * (2 + len(GROUPS)) + [vmem] * 2,
        out_specs=[hbm] * 8 + [vmem] * 2,
        scratch_shapes=[pltpu.VMEM(s.shape, s.dtype) for s in (*groups, rows, rows, *weights)]
        + [pltpu.SemaphoreType.DMA((len(GROUPS) + 2,)), pltpu.SemaphoreType.DMA((14,))],
        compiler_params=pltpu.CompilerParams(vmem_limit_bytes=60 << 20),
        name="gradients",
    )(*outs)
    ggain, gshift = results[8].transpose(1, 0, 2), results[9].transpose(1, 0, 2)
    return (*results[:8], ggain, gshift)


BLOCK_CAP = 2048


def extended_2(block, sides, width):
    for axis, dim in sides:
        count = lax.axis_size(axis)
        forward = [(i, i + 1) for i in range(count - 1)]
        forward.append((count - 1, 0))
        backward = [(target, source) for source, target in forward]
        low = lax.ppermute(
            lax.slice_in_dim(block, block.shape[dim] - width, None, axis=dim), axis, forward
        )
        high = lax.ppermute(lax.slice_in_dim(block, 0, width, axis=dim), axis, backward)
        block = jnp.concatenate([low, block, high], axis=dim)
    return block


def block_length(total_rows, upper_limit):
    for length in range(min(total_rows, upper_limit), 0, -1):
        if total_rows % length == 0:
            return length
    return 1


def outer_product(left, right):
    return lax.dot_general(
        left, right, (((0,), (0,)), ((), ())), preferred_element_type=jnp.float32
    )


def times_transposed(left, weight):
    return lax.dot_general(
        left, weight, (((1,), (1,)), ((), ())), preferred_element_type=jnp.float32
    )


def forward_product(left, weight):
    return jnp.dot(left, weight, preferred_element_type=jnp.float32)


def silu_slope_plain(inputs):
    logistic = jax.nn.sigmoid(inputs)
    return logistic * (1.0 + inputs * (1.0 - logistic))


def normalize(inputs, gain_row, shift_row, node_total):
    batch_mean = lax.psum(jnp.sum(inputs, 0), ("nodes", "rep")) / node_total
    centred = inputs - batch_mean
    batch_var = lax.psum(jnp.sum(centred * centred, 0), ("nodes", "rep")) / node_total
    inv_std = lax.rsqrt(batch_var + NORM_EPS)
    standard = (inputs - batch_mean) * inv_std
    return (standard * gain_row + shift_row, standard, inv_std)


def normalize_back(grad_out, standard, inv_std, gain_row, node_total):
    shift_grad, gain_grad = lax.psum(
        (jnp.sum(grad_out, 0), jnp.sum(grad_out * standard, 0)), ("nodes", "rep")
    )
    grad_in = (
        gain_row
        * inv_std
        * (grad_out - shift_grad / node_total - standard * gain_grad / node_total)
    )
    return (grad_in, gain_grad, shift_grad)


def exchange_sources(outgoing):
    halo_rows = outgoing.shape[0] // 2
    grown = extended_2(outgoing, (("nodes", 0),), halo_rows)
    return jnp.concatenate([grown[:halo_rows], grown[3 * halo_rows :]], 0)


def return_sources(incoming_grad):
    halo_rows = incoming_grad.shape[0] // 2
    grown = extended_2(incoming_grad.astype(jnp.bfloat16), (("nodes", 0),), halo_rows).astype(
        incoming_grad.dtype
    )
    return jnp.concatenate([grown[:halo_rows], grown[3 * halo_rows :]], 0)


def attend_forward(query_rows, key_rows, value_rows, local_graphs, group_graphs):
    row_count = query_rows.shape[0]
    score_scale = HEAD_DIM ** (-0.5)
    queries = query_rows.reshape(row_count, HEADS, HEAD_DIM)

    def add_piece(carried, kv_piece, first_row):
        key_piece, value_piece = kv_piece
        piece_rows = key_piece.shape[0]
        block_len = block_length(piece_rows, BLOCK_CAP)

        def add_block(block_state, block_index):
            row_max, row_sum, accumulated = block_state
            block_start = block_index * block_len
            key_block = lax.dynamic_slice_in_dim(key_piece, block_start, block_len, 0).reshape(
                block_len, HEADS, HEAD_DIM
            )
            value_block = lax.dynamic_slice_in_dim(value_piece, block_start, block_len, 0).reshape(
                block_len, HEADS, HEAD_DIM
            )
            key_graphs = lax.dynamic_slice_in_dim(
                group_graphs, first_row + block_start, block_len, 0
            )
            same_graph = (local_graphs[:, None] == key_graphs[None, :])[None]
            scores = (
                jnp.einsum("qhd,khd->hqk", queries, key_block, preferred_element_type=jnp.float32)
                * score_scale
            )
            scores = jnp.where(same_graph, scores, NEG)
            new_max = jnp.maximum(row_max, jnp.max(scores, 2))
            weights = jnp.where(same_graph, jnp.exp(scores - new_max[:, :, None]), 0.0)
            factor = jnp.exp(row_max - new_max)
            row_sum = row_sum * factor + jnp.sum(weights, 2)
            contrib = jnp.einsum(
                "hqk,khd->qhd",
                weights.astype(jnp.bfloat16),
                value_block,
                preferred_element_type=jnp.float32,
            )
            accumulated = accumulated * jnp.transpose(factor)[:, :, None] + contrib
            return ((new_max, row_sum, accumulated), None)

        carried, _ = lax.scan(add_block, carried, jnp.arange(piece_rows // block_len))
        return carried

    start_state = (
        jnp.full((HEADS, row_count), NEG, jnp.float32),
        jnp.zeros((HEADS, row_count), jnp.float32),
        jnp.zeros((row_count, HEADS, HEAD_DIM), jnp.float32),
    )
    row_max, row_sum, accumulated = add_piece(
        start_state,
        (
            lax.all_gather(key_rows, "nodes", axis=0, tiled=True),
            lax.all_gather(value_rows, "nodes", axis=0, tiled=True),
        ),
        jnp.int32(0),
    )
    attn_raw = accumulated / jnp.transpose(row_sum)[:, :, None]
    log_sum = row_max + jnp.log(row_sum)
    return (attn_raw, log_sum)


def attend_backward(
    query_rows, key_rows, value_rows, grad_low, attn_raw, log_sum, local_graphs, group_graphs
):
    row_count = query_rows.shape[0]
    model_width = HEADS * HEAD_DIM
    score_scale = HEAD_DIM ** (-0.5)
    queries = query_rows.reshape(row_count, HEADS, HEAD_DIM)
    grad_heads = grad_low.reshape(row_count, HEADS, HEAD_DIM)
    row_delta = jnp.einsum("qhd,qhd->hq", grad_heads.astype(jnp.float32), attn_raw)

    def score_block(key_block, value_block, key_graphs):
        same_graph = (local_graphs[:, None] == key_graphs[None, :])[None]
        scores = (
            jnp.einsum("qhd,khd->hqk", queries, key_block, preferred_element_type=jnp.float32)
            * score_scale
        )
        attn_weights = jnp.exp(jnp.where(same_graph, scores - log_sum[:, :, None], NEG))
        grad_weights = jnp.einsum(
            "qhd,khd->hqk", grad_heads, value_block, preferred_element_type=jnp.float32
        )
        grad_scores = (attn_weights * (grad_weights - row_delta[:, :, None])).astype(jnp.bfloat16)
        return (attn_weights, grad_scores)

    def key_terms(attn_weights, grad_scores, block_len):
        grad_keys = (
            jnp.einsum("hqk,qhd->khd", grad_scores, queries, preferred_element_type=jnp.float32)
            * score_scale
        )
        grad_values = jnp.einsum(
            "hqk,qhd->khd",
            attn_weights.astype(jnp.bfloat16),
            grad_heads,
            preferred_element_type=jnp.float32,
        )
        return jnp.concatenate(
            [
                grad_keys.reshape(block_len, model_width),
                grad_values.reshape(block_len, model_width),
            ],
            1,
        )

    def query_term(grad_scores, key_block):
        return (
            jnp.einsum("hqk,khd->qhd", grad_scores, key_block, preferred_element_type=jnp.float32)
            * score_scale
        )

    group_rows = group_graphs.shape[0]

    def add_piece(carried, kv_piece, first_row):
        key_piece, value_piece = kv_piece
        piece_rows = key_piece.shape[0]
        block_len = block_length(piece_rows, BLOCK_CAP)

        def add_block(block_state, block_index):
            grad_query, buffer = block_state
            block_start = block_index * block_len
            key_block = lax.dynamic_slice_in_dim(key_piece, block_start, block_len, 0).reshape(
                block_len, HEADS, HEAD_DIM
            )
            value_block = lax.dynamic_slice_in_dim(value_piece, block_start, block_len, 0).reshape(
                block_len, HEADS, HEAD_DIM
            )
            place = first_row + block_start
            key_graphs = lax.dynamic_slice_in_dim(group_graphs, place, block_len, 0)
            attn_weights, grad_scores = score_block(key_block, value_block, key_graphs)
            grad_query = grad_query + query_term(grad_scores, key_block)
            block_terms = key_terms(attn_weights, grad_scores, block_len)
            current = lax.dynamic_slice_in_dim(buffer, place, block_len, 0)
            buffer = lax.dynamic_update_slice_in_dim(buffer, current + block_terms, place, 0)
            return ((grad_query, buffer), None)

        carried, _ = lax.scan(add_block, carried, jnp.arange(piece_rows // block_len))
        return carried

    start_state = (
        jnp.zeros((row_count, HEADS, HEAD_DIM), jnp.float32),
        jnp.zeros((group_rows, 2 * model_width), jnp.float32),
    )
    grad_query, buffer = add_piece(
        start_state,
        (
            lax.all_gather(key_rows, "nodes", axis=0, tiled=True),
            lax.all_gather(value_rows, "nodes", axis=0, tiled=True),
        ),
        jnp.int32(0),
    )
    grad_kv = lax.psum_scatter(buffer, "nodes", scatter_dimension=0, tiled=True)
    return (
        grad_query.reshape(row_count, model_width),
        grad_kv[:, :model_width],
        grad_kv[:, model_width:],
    )


def layer_forward(
    hidden, params, edge_feat, edge_src, edge_dst, halo_send, local_graphs, group_graphs, node_total
):
    w_proj, w_edge, w_qkv, w_out, w_up, w_down, norm_gains, norm_shifts = params
    row_count, model_width = hidden.shape
    hidden_low = hidden.astype(jnp.bfloat16)
    projected = forward_product(hidden_low, w_proj)
    self_term = projected[:, :model_width]
    dest_term = projected[:, 2 * model_width : 3 * model_width]
    source_rows = jnp.concatenate(
        [projected[:, model_width : 2 * model_width], projected[:, 3 * model_width :]], 1
    ).astype(jnp.bfloat16)
    incoming = exchange_sources(source_rows[halo_send])
    extended = jnp.concatenate([source_rows, incoming], 0)
    edge_rows = extended[edge_src].astype(jnp.float32)
    source_b = edge_rows[:, :model_width]
    source_e = edge_rows[:, model_width:]
    edge_proj = forward_product(edge_feat, w_edge)
    gating = jax.nn.sigmoid(dest_term[edge_dst] + source_e + edge_proj)
    numerator = jax.ops.segment_sum(gating * source_b, edge_dst, row_count)
    denominator = jax.ops.segment_sum(gating, edge_dst, row_count)
    message = self_term + numerator / (denominator + GATE_EPS)
    normed_one, standard_one, inv_one = normalize(
        message, norm_gains[0], norm_shifts[0], node_total
    )
    local_out = hidden + jax.nn.silu(normed_one)
    qkv_low = forward_product(hidden_low, w_qkv).astype(jnp.bfloat16)
    query_rows = qkv_low[:, :model_width]
    key_rows = qkv_low[:, model_width : 2 * model_width]
    value_rows = qkv_low[:, 2 * model_width :]
    attn_raw, log_sum = attend_forward(query_rows, key_rows, value_rows, local_graphs, group_graphs)
    attn_low = attn_raw.reshape(row_count, model_width).astype(jnp.bfloat16)
    attn_proj = forward_product(attn_low, w_out)
    normed_two, standard_two, inv_two = normalize(
        hidden + attn_proj, norm_gains[1], norm_shifts[1], node_total
    )
    mixed = local_out + normed_two
    mixed_low = mixed.astype(jnp.bfloat16)
    up_proj = forward_product(mixed_low, w_up)
    activated = jax.nn.silu(up_proj).astype(jnp.bfloat16)
    down_proj = forward_product(activated, w_down)
    normed_three, standard_three, inv_three = normalize(
        mixed + down_proj, norm_gains[2], norm_shifts[2], node_total
    )
    saved = (
        hidden_low,
        source_b,
        gating,
        numerator,
        denominator,
        normed_one,
        standard_one,
        inv_one,
        query_rows,
        key_rows,
        value_rows,
        attn_raw,
        log_sum,
        attn_low,
        standard_two,
        inv_two,
        mixed_low,
        up_proj,
        activated,
        standard_three,
        inv_three,
    )
    return (normed_three, saved)


def layer_backward(
    grad_out,
    params,
    saved,
    edge_feat,
    edge_src,
    edge_dst,
    halo_send,
    local_graphs,
    group_graphs,
    node_total,
):
    w_proj, w_edge, w_qkv, w_out, w_up, w_down, norm_gains, norm_shifts = params
    (
        hidden_low,
        source_b,
        gating,
        numerator,
        denominator,
        normed_one,
        standard_one,
        inv_one,
        query_rows,
        key_rows,
        value_rows,
        attn_raw,
        log_sum,
        attn_low,
        standard_two,
        inv_two,
        mixed_low,
        up_proj,
        activated,
        standard_three,
        inv_three,
    ) = saved
    row_count, model_width = grad_out.shape
    grad_three, gain_three, shift_three = normalize_back(
        grad_out, standard_three, inv_three, norm_gains[2], node_total
    )
    down_grad = grad_three.astype(jnp.bfloat16)
    grad_w_down = outer_product(activated, down_grad)
    up_grad = (times_transposed(down_grad, w_down) * silu_slope_plain(up_proj)).astype(jnp.bfloat16)
    grad_w_up = outer_product(mixed_low, up_grad)
    grad_mixed = grad_three + times_transposed(up_grad, w_up)
    grad_two, gain_two, shift_two = normalize_back(
        grad_mixed, standard_two, inv_two, norm_gains[1], node_total
    )
    out_grad = grad_two.astype(jnp.bfloat16)
    grad_w_out = outer_product(attn_low, out_grad)
    attn_grad = times_transposed(out_grad, w_out).astype(jnp.bfloat16)
    grad_query, grad_key, grad_value = attend_backward(
        query_rows, key_rows, value_rows, attn_grad, attn_raw, log_sum, local_graphs, group_graphs
    )
    qkv_grad = jnp.concatenate([grad_query, grad_key, grad_value], 1).astype(jnp.bfloat16)
    grad_w_qkv = outer_product(hidden_low, qkv_grad)
    grad_message, gain_one, shift_one = normalize_back(
        grad_mixed * silu_slope_plain(normed_one), standard_one, inv_one, norm_gains[0], node_total
    )
    shifted = denominator + GATE_EPS
    grad_numer = grad_message / shifted
    grad_denom = -grad_message * numerator / (shifted * shifted)
    numer_edge = grad_numer[edge_dst]
    grad_gate = numer_edge * source_b + grad_denom[edge_dst]
    grad_pre_edge = grad_gate * gating * (1.0 - gating)
    edge_grad = grad_pre_edge.astype(jnp.bfloat16)
    grad_w_edge = outer_product(edge_feat, edge_grad)
    grad_dest = jax.ops.segment_sum(grad_pre_edge, edge_dst, row_count)
    grad_extended = jax.ops.segment_sum(
        jnp.concatenate([numer_edge * gating, grad_pre_edge], 1),
        edge_src,
        row_count + halo_send.shape[0],
    )
    returned = return_sources(grad_extended[row_count:])
    grad_source = grad_extended[:row_count].at[halo_send].add(returned)
    proj_grad = jnp.concatenate(
        [grad_message, grad_source[:, :model_width], grad_dest, grad_source[:, model_width:]], 1
    ).astype(jnp.bfloat16)
    grad_w_proj = outer_product(hidden_low, proj_grad)
    grad_hidden = (
        grad_mixed
        + grad_two
        + times_transposed(proj_grad, w_proj)
        + times_transposed(qkv_grad, w_qkv)
    )
    weight_grads = (grad_w_proj, grad_w_edge, grad_w_qkv, grad_w_out, grad_w_up, grad_w_down)
    return (
        grad_hidden,
        weight_grads,
        jnp.stack([gain_one, gain_two, gain_three]),
        jnp.stack([shift_one, shift_two, shift_three]),
    )


def per_device(
    node_input,
    edge_feat,
    graph_ids,
    edge_src,
    edge_dst,
    halo_send,
    w_proj,
    w_edge,
    w_qkv,
    w_out,
    w_up,
    w_down,
    norm_gain,
    norm_shift,
    cotangent,
):
    group_graphs = lax.all_gather(graph_ids, "nodes", axis=0, tiled=True)
    node_total = node_input.shape[0] * lax.axis_size("nodes") * lax.axis_size("rep")
    layer_count = w_proj.shape[0]
    layer_params = [
        (
            w_proj[layer_index],
            w_edge[layer_index],
            w_qkv[layer_index],
            w_out[layer_index],
            w_up[layer_index],
            w_down[layer_index],
            norm_gain[layer_index],
            norm_shift[layer_index],
        )
        for layer_index in range(layer_count)
    ]
    hidden = node_input.astype(jnp.float32)
    saved_all = []
    for layer_index in range(layer_count):
        hidden, saved = layer_forward(
            hidden,
            layer_params[layer_index],
            edge_feat,
            edge_src,
            edge_dst,
            halo_send,
            graph_ids,
            group_graphs,
            node_total,
        )
        saved_all.append(saved)
    grad_hidden = cotangent.astype(jnp.float32)
    weight_parts = [None] * layer_count
    gain_parts = [None] * layer_count
    shift_parts = [None] * layer_count
    for layer_index in range(layer_count - 1, -1, -1):
        (
            grad_hidden,
            weight_parts[layer_index],
            gain_parts[layer_index],
            shift_parts[layer_index],
        ) = layer_backward(
            grad_hidden,
            layer_params[layer_index],
            saved_all[layer_index],
            edge_feat,
            edge_src,
            edge_dst,
            halo_send,
            graph_ids,
            group_graphs,
            node_total,
        )
    proj_local = jnp.stack([weight_parts[layer_index][0] for layer_index in range(layer_count)])
    edge_local = jnp.stack([weight_parts[layer_index][1] for layer_index in range(layer_count)])
    qkv_local = jnp.stack([weight_parts[layer_index][2] for layer_index in range(layer_count)])
    out_local = jnp.stack([weight_parts[layer_index][3] for layer_index in range(layer_count)])
    up_local = jnp.stack([weight_parts[layer_index][4] for layer_index in range(layer_count)])
    down_local = jnp.stack([weight_parts[layer_index][5] for layer_index in range(layer_count)])
    grad_proj, grad_edge, grad_qkv, grad_out, grad_up, grad_down = lax.psum(
        (proj_local, edge_local, qkv_local, out_local, up_local, down_local), ("nodes", "rep")
    )
    return (
        hidden,
        grad_hidden,
        grad_proj,
        grad_edge,
        grad_qkv,
        grad_out,
        grad_up,
        grad_down,
        jnp.stack(gain_parts),
        jnp.stack(shift_parts),
    )


def solution(mesh):
    in_specs = (
        P(("rep", "nodes"), None),
        P(("rep", "nodes"), None),
        P(("rep", "nodes")),
        P(("rep", "nodes")),
        P(("rep", "nodes")),
        P(("rep", "nodes")),
        P(),
        P(),
        P(),
        P(),
        P(),
        P(),
        P(),
        P(),
        P(("rep", "nodes"), None),
    )
    out_specs = (
        P(("rep", "nodes"), None),
        P(("rep", "nodes"), None),
        P(),
        P(),
        P(),
        P(),
        P(),
        P(),
        P(),
        P(),
    )
    N, M = mesh.shape["nodes"], mesh.shape["rep"]
    fused = N in (4, 8) and M % 2 == 0 and 512 % (16 * N * M) == 0
    return jax.shard_map(
        functools.partial(fused_device, N, M) if fused else per_device,
        mesh=mesh, in_specs=in_specs, out_specs=out_specs, check_vma=False,
    )
```

```python
import functools
import math

import jax
import jax.numpy as jnp
from jax import lax
from jax.experimental import pallas as pl
from jax.experimental.pallas import tpu as pltpu
from jax.sharding import PartitionSpec as P

HEADS = 8
HEAD_DIM = 32
NEG = -1e30
NORM_EPS = 1e-05
GATE_EPS = 1e-06
F32, BF16, I32 = jnp.float32, jnp.bfloat16, jnp.int32
MESH = pl.DeviceIdType.MESH
SYNCS = 12
STRIP = 32
GROUPS = (
    ("early", 1, 0, 2560, ("core", "y", "nodes")),
    ("conv", 1, 0, 2560, ("core", "x", "y", "z")),
    ("qkv", 1, 0, 1536, ("core", "y", "nodes")),
    ("early", 0, 0, 2560, ("core", "x", "y", "z")),
    ("conv", 0, 0, 2560, ("core", "y", "nodes")),
    ("qkv", 0, 0, 1024, ("rep", "nodes")),
    ("qkv", 0, 1024, 512, ("nodes", "rep")),
)


def dot(left, right):
    return lax.dot_general(
        left, right, (((1,), (0,)), ((), ())), preferred_element_type=F32
    )


def dot_nt(left, right):
    return lax.dot_general(
        left, right, (((1,), (1,)), ((), ())), preferred_element_type=F32
    )


def dot_tn(left, right):
    return lax.dot_general(
        left, right, (((0,), (0,)), ((), ())), preferred_element_type=F32
    )


def split(value):
    high = value.astype(BF16)
    return high, (value - high.astype(F32)).astype(BF16)


def sigmoid(value):
    return jax.nn.sigmoid(value)


def silu_slope(value):
    logistic = sigmoid(value)
    return logistic * (1.0 + value * (1.0 - logistic))


def col_sum(value):
    return jnp.sum(value, axis=0, keepdims=True)


def pack(first, second):
    return jnp.concatenate([first[:, :128], first[:, 128:], second[:, :128], second[:, 128:]], 0)


def unpack(tile):
    return [jnp.concatenate([tile[i : i + 1], tile[i + 1 : i + 2]], 1) for i in (0, 2)]


def combine_moments(tiles, count):
    mean = jnp.mean(tiles[:, 0:2], 0)
    off = tiles[:, 0:2] - mean
    return jnp.concatenate([mean, jnp.sum(tiles[:, 2:4] + count * off * off, 0)], 0)


class Refs:
    pass


def axis_sizes(N, M):
    return dict(core=2, y=M // 2, x=2, z=N // 2, rep=M, nodes=N)


def scratch_list(N, M, L, R, E):
    NZ, NB, G = N // 2, N // 4, N * R
    D, FF, W, HH = 256, 512, 4 * R, HEADS // 2 * R
    dma = lambda *shape: pltpu.SemaphoreType.DMA(shape)
    vm = lambda dtype, *shape: pltpu.VMEM(shape, dtype)
    names = dict(
        gb=vm(BF16, L, N, R, D),
        xs=vm(BF16, L, N, R, D),
        meta=vm(I32, N, 8, 256),
        cot=vm(BF16, R, D),
        wp=vm(BF16, L, D, 4 * D),
        we=vm(BF16, L, D, D),
        wqkv=vm(BF16, L, D, 3 * D),
        wo=vm(BF16, L, D, D),
        wu=vm(BF16, L, D, FF),
        wd=vm(BF16, L, FF, D),
        st1=vm(F32, SYNCS, M * N, 4, 128),
        gain=vm(F32, L, 8, D),
        shift=vm(F32, L, 8, D),
        ggain=vm(F32, L, 8, D),
        gshift=vm(F32, L, 8, D),
        iv=vm(F32, L, 8, D),
        moff=vm(F32, N, 8, D),
        move=vm(F32, 8, D),
        le=vm(BF16, E, 1024),
        re=vm(BF16, 1024, D),
        TT=vm(BF16, R, 2 * E),
        ST=vm(BF16, 256, E),
        efT=vm(BF16, D, E),
        HP=vm(BF16, 32, R),
        HN=vm(BF16, 32, R),
        A=vm(BF16, R, 64),
        bias=vm(F32, R, G),
        xf=vm(F32, L + 1, R, D),
        xe=vm(BF16, L, 256, D),
        xeT=vm(BF16, D, 256),
        gate=vm(F32, L, E, D),
        bs=vm(BF16, L, E, D),
        num=vm(F32, L, R, D),
        den=vm(F32, L, R, D),
        z0=vm(F32, L, R, D),
        z1=vm(F32, L, R, D),
        z2=vm(F32, L, R, D),
        wkvT=vm(BF16, L, 2 * D, D),
        kvT=vm(BF16, L, 2 * D, G),
        odT=vm(F32, NB, D, R),
        ldT=vm(F32, NB, D, R),
        md=vm(F32, NB, R, D),
        rb=vm(F32, L, NB, R, D),
        pst=vm(BF16, L, HEADS * R, G),
        oraw=vm(F32, L, R, D),
        ob=vm(BF16, L, R, D),
        mb=vm(BF16, L, R, D),
        u=vm(F32, L, R, FF),
        g=vm(BF16, L, R, FF),
        dy=vm(F32, R, D),
        dmix=vm(F32, R, D),
        gy0=vm(F32, R, D),
        local=vm(F32, R, D),
        dxo=vm(F32, R, D),
        dob=vm(F32, R, D),
        dqT=vm(F32, D, R),
        qm=vm(BF16, L, 2, HH, 128),
        q=vm(BF16, L, R, D),
        qT=vm(BF16, D, R),
        dosT=vm(BF16, 128, R),
        dom=vm(BF16, HH, 256),
        sc=vm(F32, 2, max(2 * R, E), W),
        tp=vm(F32, HEADS // 2, R, 128),
        dss=vm(BF16, HH, W),
        dkv=vm(BF16, 2 * D, W),
        gkv=vm(F32, 2 * D, D),
        gg=vm(BF16, 2 * E, 2 * D),
        dn=vm(BF16, 512, 2 * D),
        dproj=vm(BF16, 256, 4 * D),
        dxs=vm(BF16, L, NZ, 2, R, D),
        rs1=vm(BF16, L, NZ, R, D),
        cs=vm(BF16, L, NZ, R, D),
        rs2=vm(BF16, L, NZ, R, D),
        ro=vm(BF16, L, 3, R, D),
        hs=vm(BF16, L, 2, 32, D),
        hr=vm(BF16, L, 2, 32, D),
    )
    names.update(
        gs_early=vm(BF16, L, 2560, 128),
        gs_conv=vm(BF16, L, 2560, 128),
        gs_qkv=vm(BF16, L, 1536, 128),
    )
    sizes = axis_sizes(N, M)
    for g, (_, _, _, rows, stages) in enumerate(GROUPS):
        names[f"go{g}"] = vm(BF16, rows, 128)
        left = rows
        for k, axis in enumerate(stages):
            left //= sizes[axis]
            names[f"ga{g}_{k}"] = vm(BF16, sizes[axis] - 1, left, 128)
            if k < len(stages) - 1:
                names[f"gh{g}_{k}"] = vm(BF16, left, 128)
    names.update(
        ar_s=dma(len(GROUPS), 8),
        ar_r=dma(len(GROUPS), 8),
        ar_l=dma(len(GROUPS)),
        load=dma(10),
        store=dma(2),
        meta_s=dma(1),
        meta_r=dma(1),
        st1_s=dma(SYNCS),
        st1_r=dma(SYNCS),
        agc_s=dma(L, NZ),
        agc_r=dma(L, NZ),
        agp_s=dma(L, NZ),
        agp_r=dma(L, NZ),
        rsp_s=dma(L, NZ),
        rsp_r=dma(L, NZ),
        ro_s=dma(L, 3),
        ro_r=dma(L, 3),
        rsc_s=dma(L, NZ),
        rsc_r=dma(L, NZ),
        hal_s=dma(L, 2),
        hal_r=dma(L, 2),
    )
    return names


IN_NAMES = (
    "x_in", "ids", "edge_src", "edge_dst", "halo", "ef_h", "wp_h", "we_h", "wqkv_h", "wo_h", "wu_h", "wd_h",
    "gain_in", "shift_in", "cot_h",
)
OUT_NAMES = ("out_act", "grad_in", *(f"gout{g}" for g in range(len(GROUPS))), "ggain_out", "gshift_out")


def kernel(N, M, L, names, *args):
    r_ = Refs()
    for name, ref in zip(IN_NAMES + OUT_NAMES + tuple(names), args, strict=True):
        setattr(r_, name, ref)
    R, D = r_.x_in.shape
    E = r_.ef_h.shape[0]
    NZ, NB, G, W = N // 2, N // 4, N * R, 4 * R
    HK = HEADS // 2
    total = float(N * M * R)
    scale = HEAD_DIM ** -0.5
    me = lax.axis_index("nodes")
    rep = lax.axis_index("rep")
    z = me // 2
    par = me % 2
    partner = 2 * z + (1 - par)
    prev = (me + N - 1) % N
    nxt = (me + 1) % N
    zh, zl = z // 2, z % 2
    z_to = lambda t: 2 * ((zh + t // 2) % NB) + (zl + t % 2) % 2
    z_from = lambda t: 2 * ((zh + NB - t // 2) % NB) + (zl + t % 2) % 2

    def remote(src, dst, s_sem, r_sem, **where):
        return pltpu.make_async_remote_copy(
            src_ref=src, dst_ref=dst, send_sem=s_sem, recv_sem=r_sem,
            device_id=where, device_id_type=MESH,
        )

    def send(src, dst, s_sem, r_sem, **where):
        remote(src, dst, s_sem, r_sem, **where).start()

    def send_rows(src, dst, rows, s_sem, r_sem, **where):
        pieces = next(p for p in range(1, rows) if rows % (16 * p) == 0 and rows // p <= 128)
        for at in range(0, rows, rows // pieces):
            cut = pl.ds(at, rows // pieces)
            send(src.at[cut], dst.at[cut], s_sem, r_sem, **where)

    def arrive(dst, r_sem):
        remote(dst, dst, r_sem, r_sem, nodes=partner).wait_recv()

    def sent(src, s_sem):
        remote(src, src, s_sem, s_sem, nodes=partner).wait_send()

    def when(condition, *acts):
        @pl.when(condition)
        def _():
            for act in acts:
                act()

    loads = [pltpu.make_async_copy(r_.ef_h, r_.le.at[:, D : 2 * D], r_.load.at[0])] + [
        pltpu.make_async_copy(getattr(r_, f"{name}_h"), getattr(r_, name), r_.load.at[1 + i])
        for i, name in enumerate(("we", "wqkv", "wp", "wo", "wu", "wd", "cot"))
    ]
    own_rows = pltpu.make_async_copy(r_.x_in, r_.gb.at[0, me], r_.load.at[8])
    own_rows.start()
    for load in loads:
        load.start()

    barrier = pltpu.get_barrier_semaphore()
    for dr in range(M):
        for d in range(N):
            if dr + d > 0:
                pl.semaphore_signal(barrier, inc=1, device_id={"rep": (rep + dr) % M, "nodes": (me + d) % N},
                                    device_id_type=MESH)
    pl.semaphore_wait(barrier, M * N - 1)

    def gather_start(l):
        mine = r_.gb.at[l, me]
        send_rows(mine, mine, R, r_.agp_s.at[l, 0], r_.agp_r.at[l, 0], nodes=partner)
        send_rows(mine, mine, R, r_.agc_s.at[l, 1], r_.agc_r.at[l, 1], nodes=2 * z_to(1) + par)
        send_rows(mine, mine, R, r_.agp_s.at[l, 1], r_.agp_r.at[l, 1], nodes=2 * z_to(1) + 1 - par)
        for t in range(2, NZ):
            send_rows(mine, mine, R, r_.agc_s.at[l, t], r_.agc_r.at[l, t], nodes=2 * z_to(t) + par)

    def gather_pass(l, t):
        piece = r_.gb.at[l, 2 * z_from(t) + par]
        arrive(piece, r_.agc_r.at[l, t])
        send_rows(piece, piece, R, r_.agp_s.at[l, t], r_.agp_r.at[l, t], nodes=partner)

    def gather_take(l, t):
        arrive(r_.gb.at[l, 2 * z_from(t) + 1 - par], r_.agp_r.at[l, t])

    def sync_start(k, first, second):
        mine = rep * N + me
        r_.st1[k, mine] = pack(first, second)
        for dr in range(M):
            for d in range(N):
                if dr + d > 0:
                    send(r_.st1.at[k, mine], r_.st1.at[k, mine], r_.st1_s.at[k], r_.st1_r.at[k],
                         rep=(rep + dr) % M, nodes=(me + d) % N)

    def sync_wait(k):
        arrive(r_.st1.at[k, 0 : M * N - 1], r_.st1_r.at[k])

    def sync_moments(k):
        sync_wait(k)
        return unpack(combine_moments(r_.st1[k], float(R)))

    def sync_sums(k):
        sync_wait(k)
        return unpack(jnp.sum(r_.st1[k], 0))

    sizes = axis_sizes(N, M)
    core, row = rep % 2, rep // 2
    places = dict(
        core=(core, lambda t: dict(rep=2 * row + t)),
        y=(row, lambda t: dict(rep=2 * t + core)),
        x=(par, lambda t: dict(nodes=2 * z + t)),
        z=(z, lambda t: dict(nodes=2 * t + par)),
        rep=(rep, lambda t: dict(rep=t)),
        nodes=(me, lambda t: dict(nodes=t)),
    )

    def reduce_step(g, step):
        name, layer, first, rows, stages = GROUPS[g]
        K = len(stages)
        gs, out = getattr(r_, f"gs_{name}").at[layer, first : first + rows], getattr(r_, f"go{g}")
        count, offset = [rows], [0]
        for axis in stages:
            count.append(count[-1] // sizes[axis])
            offset.append(offset[-1] + places[axis][0] * count[-1])
        take = lambda start, size: pl.ds(pl.multiple_of(start, 16), size)
        if 1 <= step <= K:
            k = step - 1
            got = getattr(r_, f"ga{g}_{k}")
            arrive(got, r_.ar_r.at[g, k])
            held = gs if k == 0 else getattr(r_, f"gh{g}_{k - 1}")
            index = places[stages[k]][0]
            acc = held[take(index * count[k + 1], count[k + 1])].astype(F32)
            for slot in range(sizes[stages[k]] - 1):
                acc = acc + got[slot].astype(F32)
            if step < K:
                getattr(r_, f"gh{g}_{k}")[...] = acc.astype(BF16)
            else:
                out[take(offset[K], count[K])] = acc.astype(BF16)
        elif step > K:
            k = 2 * K - step
            arrive(out.at[0 : (sizes[stages[k]] - 1) * count[k + 1]], r_.ar_r.at[g, step - 1])
        if step < K:
            held = gs if step == 0 else getattr(r_, f"gh{g}_{step - 1}")
            index, device = places[stages[step]]
            size = sizes[stages[step]]
            for d in range(1, size):
                to = (index + d) % size
                send_rows(held.at[take(to * count[step + 1], count[step + 1])], getattr(r_, f"ga{g}_{step}").at[d - 1],
                     count[step + 1], r_.ar_s.at[g, step], r_.ar_r.at[g, step], **device(to))
        elif step < 2 * K:
            k = 2 * K - 1 - step
            index, device = places[stages[k]]
            size = sizes[stages[k]]
            here = out.at[take(offset[k + 1], count[k + 1])]
            for d in range(1, size):
                send_rows(here, here, count[k + 1], r_.ar_s.at[g, step], r_.ar_r.at[g, step],
                          **device((index + d) % size))
        else:
            pltpu.make_async_copy(out, getattr(r_, f"gout{g}"), r_.ar_l.at[g]).start()

    def reduce_drain(g):
        _, _, _, rows, stages = GROUPS[g]
        K, left = len(stages), rows
        out = getattr(r_, f"go{g}")
        for k, axis in enumerate(stages):
            left //= sizes[axis]
            for step in (k, 2 * K - 1 - k):
                sent(out.at[0 : (sizes[axis] - 1) * left], r_.ar_s.at[g, step])
        pltpu.make_async_copy(out, getattr(r_, f"gout{g}"), r_.ar_l.at[g]).wait()

    def put(buf, l, at, value):
        rows = value.shape[0]
        for c in range(value.shape[1] // 128):
            buf[l, at : at + rows] = value[:, 128 * c : 128 * (c + 1)].astype(BF16)
            at += rows
        return at

    lane_head = lax.broadcasted_iota(I32, (R, 128), 1) // HEAD_DIM

    def by_head(parts):
        out = parts[0]
        for k in range(1, HK):
            out = jnp.where(lane_head == k, parts[k], out)
        return out

    r_.meta[me] = jnp.full((8, 256), -1, I32)
    r_.meta[me, 0:1, 0:R] = r_.ids[...].reshape(1, R)
    r_.meta[me, 1:2, 0:48] = r_.halo[...].reshape(1, 48)
    for d in range(1, N):
        send(r_.meta.at[me], r_.meta.at[me], r_.meta_s.at[0], r_.meta_r.at[0], nodes=(me + d) % N)
    own_rows.wait()
    gather_start(0)

    src_row = r_.edge_src[...].reshape(1, E)
    src_row = jnp.where(src_row < R + 24, src_row, src_row + 8)
    dst_row = r_.edge_dst[...].reshape(1, E)
    src_col = jnp.broadcast_to(src_row, (128, E)).T[:, 0:1]
    dst_col = jnp.broadcast_to(dst_row, (128, E)).T[:, 0:1]
    as_mask = lambda cond: cond.astype(F32).astype(BF16)
    r_.le[:, 0:256] = as_mask(src_col == lax.broadcasted_iota(I32, (E, 256), 1))
    target = as_mask(dst_col == lax.broadcasted_iota(I32, (E, 256), 1))
    r_.le[:, 512:768] = target
    r_.le[:, 768:1024] = target
    target = as_mask(dst_row == lax.broadcasted_iota(I32, (R, E), 0))
    r_.TT[:, 0:E] = target
    r_.TT[:, E:] = target
    r_.ST[...] = as_mask(src_row == lax.broadcasted_iota(I32, (256, E), 0))
    r_.dn[R:256] = jnp.zeros((256 - R, 2 * D), BF16)
    r_.dn[256 + R : 512] = jnp.zeros((256 - R, 2 * D), BF16)
    r_.dproj[R:256, 0:D] = jnp.zeros((256 - R, D), BF16)
    r_.dproj[R:256, 2 * D : 3 * D] = jnp.zeros((256 - R, D), BF16)
    loads[0].wait()
    r_.efT[...] = r_.le[:, D : 2 * D].T
    for l in range(L):
        for k in range(3):
            r_.gain[l, k : k + 1] = r_.gain_in[k, l : l + 1]
            r_.shift[l, k : k + 1] = r_.shift_in[k, l : l + 1]
    r_.xf[0] = r_.gb[0, me].astype(F32)
    r_.moff[...] = jnp.zeros((N, 8, D), F32)
    r_.move[0:1] = jnp.ones((1, D), F32)
    r_.move[1:2] = jnp.zeros((1, D), F32)
    for load in loads[1:]:
        load.wait()
    for l in range(L):
        r_.wkvT[l] = r_.wqkv[l, :, D:].T

    arrive(r_.meta.at[0 : N - 1], r_.meta_r.at[0])
    id_col = jnp.broadcast_to(r_.meta[me][0:1, 0:R], (128, R)).T[:, 0:1]
    id_row = jnp.concatenate([r_.meta[j][0:1, 0:R] for j in range(N)], 1)
    r_.bias[...] = jnp.where(id_col == id_row, 0.0, NEG)

    def halo_onehot(device, start):
        col = jnp.broadcast_to(r_.meta[device][1:2, 0:128], (128, 128)).T[start : start + 24, 0:1]
        hot = (col == lax.broadcasted_iota(I32, (24, R), 1)).astype(F32)
        return jnp.concatenate([hot, jnp.zeros((8, R), F32)], 0).astype(BF16)

    r_.HP[...] = halo_onehot(prev, 24)
    r_.HN[...] = halo_onehot(nxt, 0)
    r_.A[...] = as_mask(r_.meta[me][1:2, 0:64] == lax.broadcasted_iota(I32, (R, 64), 0))

    factor_exp = scale * math.log2(math.e)

    def prepare_queries(l):
        q = dot(r_.xs[l, me], r_.wqkv[l, :, :D]).astype(BF16)
        r_.q[l] = q
        q = q.astype(F32)
        for hf in range(2):
            for k in range(HK):
                part = jnp.where(lane_head == k, q[:, 128 * hf : 128 * (hf + 1)], 0.0)
                r_.qm[l, hf, k * R : (k + 1) * R] = part.astype(BF16)

    def head_dims(hf, k, base=0):
        return pl.ds(pl.multiple_of(base + hf * 128 + k * HEAD_DIM, HEAD_DIM), HEAD_DIM)

    def head_rows(hf, k, count=1):
        return pl.ds(pl.multiple_of((hf * HK + k) * R, 64), count * R)

    def lane_half(hf):
        return pl.ds(pl.multiple_of(hf * 128, 128), 128)

    def half_of(i):
        half = (zh + NB - i) % NB
        return half, pl.ds(pl.multiple_of(half * W, 128), W)

    def attention_keys(l, i):
        half, rows = half_of(i)
        x = r_.xs[l, pl.ds(4 * half, 4)].reshape(W, D)
        r_.kvT[l, :, rows] = dot_nt(r_.wkvT[l], x).astype(BF16)

    def attention_heads(l, i, hfs):
        _, rows = half_of(i)
        for hf in hfs:
            lanes = lane_half(hf)
            ones = jnp.ones((HEAD_DIM, W), BF16)
            for c in range(HK // 2):
                r_.sc[c % 2, 0 : 2 * R] = dot(r_.qm[l, hf, 2 * c * R : 2 * (c + 1) * R], r_.kvT[l, lanes, rows])
                for k in range(2):
                    for at in range(0, R, STRIP):
                        s = r_.sc[c % 2, k * R + at : k * R + at + STRIP] + r_.bias[at : at + STRIP, rows]
                        top = jnp.max(s, 1, keepdims=True)
                        e = jnp.exp2((s - top) * factor_exp)
                        r_.tp[2 * c + k, at : at + STRIP] = jnp.broadcast_to(top, (STRIP, 128))
                        first = pl.multiple_of((hf * HK + 2 * c + k) * R + at, STRIP)
                        r_.pst[l, pl.ds(first, STRIP), rows] = e.astype(BF16)
                for k in range(2):
                    h = 2 * c + k
                    left = jnp.concatenate([r_.kvT[l, head_dims(hf, h, D), rows], ones], 0)
                    o = dot_nt(left, r_.pst[l, head_rows(hf, h), rows])
                    r_.odT[i, head_dims(hf, h)] = o[0:HEAD_DIM]
                    r_.ldT[i, head_dims(hf, h)] = o[HEAD_DIM:]
            r_.md[i, :, lanes] = by_head([r_.tp[k] for k in range(HK)])

    def attention_end(l):
        tops = [r_.md[i].T for i in range(NB)]
        top = tops[0]
        for i in range(1, NB):
            top = jnp.maximum(top, tops[i])
        factors = [jnp.exp2((tops[i] - top) * factor_exp) for i in range(NB)]
        inv = 1.0 / sum(factors[i] * r_.ldT[i] for i in range(NB))
        o = jnp.zeros((D, R), F32)
        for i in range(NB):
            r_.rb[l, i] = (factors[i] * inv).T
            o = o + factors[i] * inv * r_.odT[i]
        o = o.T
        r_.oraw[l] = o
        ob = o.astype(BF16)
        r_.ob[l] = ob
        t1 = r_.xf[l] + dot(ob, r_.wo[l])
        r_.z1[l] = t1
        mean1 = col_sum(t1) / R
        return mean1, col_sum((t1 - mean1) * (t1 - mean1))

    def convolution(l):
        xs = r_.xs
        xb = xs[l, me]
        r_.xe[l, 0:R] = xb
        r_.xe[l, R : R + 32] = dot(r_.HP[...], xs[l, prev]).astype(BF16)
        r_.xe[l, R + 32 : R + 64] = dot(r_.HN[...], xs[l, nxt]).astype(BF16)
        xe = r_.xe[l]
        made = dot(xe, r_.wp[l])
        pd_high, pd_low = split(made[:, 2 * D : 3 * D])
        r_.re[0:256] = made[:, 3 * D :].astype(BF16)
        r_.re[256:512] = r_.we[l]
        r_.re[512:768] = pd_high
        r_.re[768:1024] = pd_low
        r_.gate[l] = dot(r_.le[...], r_.re[...])
        r_.bs[l] = dot(r_.le[:, 0:256], made[:, D : 2 * D].astype(BF16)).astype(BF16)
        for at in range(0, E, 64):
            here = slice(at, at + 64)
            gate = sigmoid(r_.gate[l, here])
            r_.gate[l, here] = gate
            high, low = split(jnp.concatenate([gate * r_.bs[l, here].astype(F32), gate], 1))
            r_.gg[here] = high
            r_.gg[E + at : E + at + 64] = low
        num_den = dot(r_.TT[...], r_.gg[...])
        pa, num, den = made[0:R, 0:D], num_den[:, 0:D], num_den[:, D:]
        r_.num[l] = num
        r_.den[l] = den
        msg = pa + num / (den + GATE_EPS)
        r_.z0[l] = msg
        mean0 = col_sum(msg) / R
        return mean0, col_sum((msg - mean0) * (msg - mean0))

    def forward(l, carry):
        def ready(js):
            for j in js:
                moved = (r_.gb[l, j].astype(F32) + r_.moff[j, 0:1]) * r_.move[0:1] + r_.move[1:2]
                r_.xs[l, j] = moved.astype(BF16)

        r_.xs[l, me] = r_.xf[l].astype(BF16)
        prepare_queries(l)
        arrive(r_.gb.at[l, 2 * z_from(1) + par], r_.agc_r.at[l, 1])
        gather_take(l, 0)
        gather_take(l, 1)
        ready([partner, 2 * z_from(1) + par, 2 * z_from(1) + 1 - par])

        attention_keys(l, 0)
        attention_heads(l, 0, (0,))
        for t in range(2, NZ):
            gather_pass(l, t)
        attention_heads(l, 0, (1,))
        for t in range(2, NZ):
            gather_take(l, t)
        ready([2 * z_from(t) + p for t in range(2, NZ) for p in range(2)])
        mean0, sq0 = convolution(l)
        for i in range(1, NB):
            attention_keys(l, i)
            attention_heads(l, i, (0, 1))
        sync_start(3 * l, mean0, sq0)
        mean1, sq1 = attention_end(l)
        sync_start(3 * l + 1, mean1, sq1)
        mean0, sq0 = sync_moments(3 * l)
        inv0 = lax.rsqrt(sq0 / total + NORM_EPS)
        r_.iv[l, 0:1] = inv0
        z0 = (r_.z0[l] - mean0) * inv0
        r_.z0[l] = z0
        n0 = z0 * r_.gain[l, 0:1] + r_.shift[l, 0:1]
        r_.local[...] = r_.xf[l] + n0 * sigmoid(n0)
        mean1, sq1 = sync_moments(3 * l + 1)
        inv1 = lax.rsqrt(sq1 / total + NORM_EPS)
        r_.iv[l, 1:2] = inv1
        z1 = (r_.z1[l] - mean1) * inv1
        r_.z1[l] = z1
        mix = r_.local[...] + z1 * r_.gain[l, 1:2] + r_.shift[l, 1:2]
        mb = mix.astype(BF16)
        r_.mb[l] = mb
        u = dot(mb, r_.wu[l])
        r_.u[l] = u
        g = (u * sigmoid(u)).astype(BF16)
        r_.g[l] = g
        y = mix + dot(g, r_.wd[l])
        r_.z2[l] = y
        mean = col_sum(y) / R
        cent = y - mean
        k = 3 * l + 2
        sync_start(k, mean, col_sum(cent * cent))

        @pl.when(l < L - 1)
        def _():
            r_.gb[l + 1, me] = cent.astype(BF16)
            gather_start(l + 1)

        @pl.when(l == L - 1)
        def _():
            dy = r_.cot[...].astype(F32)
            sync_start(3 * L, col_sum(dy), col_sum(dy * cent))

        tot_mean, tot_sq = sync_moments(k)
        inv2 = lax.rsqrt(tot_sq / total + NORM_EPS)
        r_.iv[l, 2:3] = inv2
        z2 = (r_.z2[l] - tot_mean) * inv2
        r_.z2[l] = z2
        gain, shift = r_.gain[l, 2:3], r_.shift[l, 2:3]
        r_.xf[l + 1] = z2 * gain + shift

        @pl.when(l == L - 1)
        def _():
            sync_wait(3 * L)
            sums, means = r_.st1[3 * L], r_.st1[k][:, 0:2]
            mean = jnp.mean(means, 0)
            dy_sum = jnp.sum(sums[:, 0:2], 0)
            dy_cent = jnp.sum(sums[:, 2:4] + (means - mean) * sums[:, 0:2], 0)
            dy_sum, dy_cent = unpack(jnp.concatenate([dy_sum, dy_cent], 0))
            r_.gshift[l, 2:3] = dy_sum
            r_.ggain[l, 2:3] = dy_cent * inv2

        for j in range(N):
            tile = r_.st1[k, rep * N + j]
            r_.moff[j, 0:1] = jnp.concatenate([tile[0:1], tile[1:2]], 1) - tot_mean
        r_.move[0:1] = inv2 * gain
        r_.move[1:2] = shift
        return carry

    lax.fori_loop(0, L, forward, 0)
    act_copy = pltpu.make_async_copy(r_.xf.at[L], r_.out_act, r_.store.at[0])
    act_copy.start()

    def back_feed_forward(l, k):
        s2, g2 = r_.gshift[l, 2:3], r_.ggain[l, 2:3]
        d3 = r_.gain[l, 2:3] * r_.iv[l, 2:3] * (r_.dy[...] - s2 / total - r_.z2[l] * (g2 / total))
        db = d3.astype(BF16)
        dub = (dot_nt(db, r_.wd[l]) * silu_slope(r_.u[l])).astype(BF16)
        dmix = d3 + dot_nt(dub, r_.wu[l])
        r_.dmix[...] = dmix
        n0 = r_.z0[l] * r_.gain[l, 0:1] + r_.shift[l, 0:1]
        gy0 = dmix * silu_slope(n0)
        sync_start(k, col_sum(dmix), col_sum(dmix * r_.z1[l]))
        sync_start(k + 1, col_sum(gy0), col_sum(gy0 * r_.z0[l]))
        r_.gy0[...] = gy0
        at = put(r_.gs_early, l, 512, dot_tn(r_.mb[l], dub))
        put(r_.gs_early, l, at, dot_tn(r_.g[l], db))
        r_.xeT[...] = r_.xe[l].T
        r_.qT[...] = r_.q[l].T

    def back_norms(l, k):
        s1, g1 = sync_sums(k)
        r_.gshift[l, 1:2] = s1
        r_.ggain[l, 1:2] = g1
        dmix = r_.dmix[...]
        d2 = r_.gain[l, 1:2] * r_.iv[l, 1:2] * (dmix - s1 / total - r_.z1[l] * (g1 / total))
        dab = d2.astype(BF16)
        r_.dxo[...] = dmix + d2
        r_.dob[...] = dot_nt(dab, r_.wo[l]).astype(BF16).astype(F32)
        put(r_.gs_early, l, 0, dot_tn(r_.ob[l], dab))
        r_.gkv[...] = jnp.zeros((2 * D, D), F32)
        r_.dqT[...] = jnp.zeros((D, R), F32)

    def back_half(i):
        t1 = (i + 1) % NB
        half = (zh + t1) % NB
        return t1, half, pl.ds(pl.multiple_of(half * W, 128), W)

    def back_heads(l, i, hf):
        t1, half, rows = back_half(i)
        if True:
            lanes = lane_half(hf)
            dos = r_.dob[:, lanes] * r_.rb[l, (NB - t1) % NB, :, lanes]
            prod = dos * r_.oraw[l, :, lanes]
            for k in range(HK):
                r_.dom[k * R : (k + 1) * R, 0:128] = jnp.where(lane_head == k, dos, 0.0).astype(BF16)
                r_.dom[k * R : (k + 1) * R, 128:256] = jnp.where(lane_head == k, -prod, 0.0).astype(BF16)
            r_.dosT[...] = dos.T.astype(BF16)
            values = pl.ds(pl.multiple_of(D + hf * 128, 128), 128)
            right = jnp.concatenate([r_.kvT[l, values, rows], jnp.ones((128, W), BF16)], 0)
            for c in range(HK // 2):
                both = slice(2 * c * R, 2 * (c + 1) * R)
                r_.sc[c % 2, 0 : 2 * R] = dot(r_.dom[both], right)
                for k in range(2):
                    for at in range(0, R, STRIP):
                        first = pl.multiple_of((hf * HK + 2 * c + k) * R + at, STRIP)
                        e = r_.pst[l, pl.ds(first, STRIP), rows].astype(F32)
                        ds = e * r_.sc[c % 2, k * R + at : k * R + at + STRIP]
                        r_.dss[(2 * c + k) * R + at : (2 * c + k) * R + at + STRIP] = ds.astype(BF16)
                for k in range(2):
                    h = 2 * c + k
                    mine, dims = slice(h * R, (h + 1) * R), head_dims(hf, h)
                    r_.dqT[dims] += dot_nt(r_.kvT[l, dims, rows], r_.dss[mine])
                    r_.dkv[dims] = (dot(r_.qT[dims], r_.dss[mine]) * scale).astype(BF16)
                    dv = dot(r_.dosT[h * HEAD_DIM : (h + 1) * HEAD_DIM], r_.pst[l, head_rows(hf, h), rows])
                    r_.dkv[head_dims(hf, h, D)] = dv.astype(BF16)

    def back_rows(l, i):
        t1, half, rows = back_half(i)
        dx = dot(r_.wqkv[l, :, D:], r_.dkv[...]).T
        r_.dxs[l, pl.ds(2 * half, 2)] = dx.astype(BF16).reshape(2, 2, R, D)

        if i < NB - 1:
            for low in range(2):
                zb = 2 * half + low
                send_rows(r_.dxs.at[l, zb, 1 - par], r_.rs1.at[l, zb], R,
                     r_.rsp_s.at[l, 2 * i + low], r_.rsp_r.at[l, 2 * i + low], nodes=partner)

        else:
            near = z_to(1)
            send_rows(r_.dxs.at[l, z, 1 - par], r_.ro.at[l, 0], R, r_.ro_s.at[l, 0], r_.ro_r.at[l, 0], nodes=partner)
            send_rows(r_.dxs.at[l, near, par], r_.ro.at[l, 1], R, r_.ro_s.at[l, 1], r_.ro_r.at[l, 1], nodes=2 * near + par)
            send_rows(r_.dxs.at[l, near, 1 - par], r_.ro.at[l, 2], R, r_.ro_s.at[l, 2], r_.ro_r.at[l, 2],
                 nodes=2 * near + 1 - par)

        r_.gkv[...] += dot(r_.dkv[...], r_.xs[l, pl.ds(4 * half, 4)].reshape(W, D))

    def pass_on(l, i, t):
        zb = z_to(t)
        arrive(r_.rs1.at[l, zb], r_.rsp_r.at[l, 2 * i + zb % 2])
        both = r_.dxs[l, zb, par].astype(F32) + r_.rs1[l, zb].astype(F32)
        r_.cs[l, zb] = both.astype(BF16)
        send_rows(r_.cs.at[l, zb], r_.rs2.at[l, z], R, r_.rsc_s.at[l, t], r_.rsc_r.at[l, t], nodes=2 * zb + par)

    def back_convolution(l, k):
        s0, g0 = unpack(jnp.sum(r_.st1[k + 1], 0))
        r_.gshift[l, 0:1] = s0
        r_.ggain[l, 0:1] = g0
        inv_den = 1.0 / (r_.den[l] + GATE_EPS)
        dm = r_.gain[l, 0:1] * r_.iv[l, 0:1] * (r_.gy0[...] - s0 / total - r_.z0[l] * (g0 / total))
        dnum = dm * inv_den
        dden = -dnum * r_.num[l] * inv_den
        high, low = split(jnp.concatenate([dnum, dden], 1))
        r_.dn[0:R] = high
        r_.dn[256 : 256 + R] = low
        r_.sc[0, 0:E, 0 : 2 * D] = dot(r_.le[:, 512:1024], r_.dn[...])
        for at in range(0, E, 64):
            here = slice(at, at + 64)
            gate, dnum_e = r_.gate[l, here], r_.sc[0, here, 0:D]
            dgp = (dnum_e * r_.bs[l, here].astype(F32) + r_.sc[0, here, D : 2 * D]) * gate * (1.0 - gate)
            r_.gg[here, 0:D] = (dnum_e * gate).astype(BF16)
            r_.gg[here, D:] = dgp.astype(BF16)
        ext = dot(r_.ST[...], r_.gg[0:E]).astype(BF16)
        r_.dproj[0:R, 0:D] = dm.astype(BF16)
        r_.dproj[:, D : 2 * D] = ext[:, 0:D]
        r_.dproj[0:R, 2 * D : 3 * D] = dot(r_.TT[:, 0:E], r_.gg[0:E, D:]).astype(BF16)
        r_.dproj[:, 3 * D :] = ext[:, D:]
        dxe = dot_nt(r_.dproj[...], r_.wp[l])
        r_.hs[l, 0] = dxe[R : R + 32].astype(BF16)
        r_.hs[l, 1] = dxe[R + 32 : R + 64].astype(BF16)
        r_.dxo[...] += dxe[0:R]

    def send_halo(l):
        send(r_.hs.at[l, 0], r_.hr.at[l, 1], r_.hal_s.at[l, 0], r_.hal_r.at[l, 0], nodes=prev)
        send(r_.hs.at[l, 1], r_.hr.at[l, 0], r_.hal_s.at[l, 1], r_.hal_r.at[l, 1], nodes=nxt)

    def conv_weight_grads(l):
        at = put(r_.gs_conv, l, 0, dot(r_.xeT[...], r_.dproj[...]))
        put(r_.gs_conv, l, at, dot(r_.efT[...], r_.gg[0:E, D:]))

    def back_input(l):
        dx = r_.dxo[...]
        dx = dx + r_.dxs[l, z, par].astype(F32)
        for slot in range(3):
            arrive(r_.ro.at[l, slot], r_.ro_r.at[l, slot])
            dx = dx + r_.ro[l, slot].astype(F32)
        for t in range(2, NZ):
            c = z_from(t)
            arrive(r_.rs2.at[l, c], r_.rsc_r.at[l, t])
            dx = dx + r_.rs2[l, c].astype(F32)
        arrive(r_.hr.at[l, 0], r_.hal_r.at[l, 1])
        arrive(r_.hr.at[l, 1], r_.hal_r.at[l, 0])
        back = jnp.concatenate(
            [r_.hr[l, 0].astype(F32)[0:24], r_.hr[l, 1].astype(F32)[0:24], jnp.zeros((16, D), F32)], 0
        )
        return dx + dot(r_.A[...], back.astype(BF16))

    r_.dy[...] = r_.cot[...].astype(F32)

    E1, C1, Q1, E0, C0, QK0, V0 = range(len(GROUPS))

    def steps(*pairs):
        return [functools.partial(reduce_step, g, k) for g, k in pairs]

    r_.dy[...] = r_.cot[...].astype(F32)

    def backward(b, carry):
        l = L - 1 - b
        first, last = b == 0, b == L - 1
        k = 3 * L + 1 + 2 * b
        back_feed_forward(l, k)
        back_norms(l, k)
        sync_wait(k + 1)
        when(first, *steps((E1, 0)))
        when(last, *steps((E1, 3), (C1, 1), (Q1, 1), (E0, 0)))
        back_convolution(l, k)
        back_heads(l, 0, 0)
        send_halo(l)
        when(first, *steps((E1, 1)))
        when(last, *steps((C1, 2), (Q1, 2), (E1, 4), (E0, 1)))
        conv_weight_grads(l)
        back_heads(l, 0, 1)
        back_rows(l, 0)
        when(first, *steps((C1, 0)))
        when(last, *steps((C0, 0), (E0, 2), (C1, 3), (Q1, 3), (E1, 5)))
        back_heads(l, 1, 0)
        for t in range(2, NZ):
            pass_on(l, 0, t)
        when(first, *steps((E1, 2)))
        when(last, *steps((E0, 3), (C0, 1), (C1, 4), (Q1, 4), (E1, 6)))
        back_heads(l, 1, 1)
        back_rows(l, 1)
        when(last, *steps((E0, 4), (C1, 5), (Q1, 5)))
        dqb = (r_.dqT[...].T * scale).astype(BF16)
        r_.dxo[...] += dot_nt(dqb, r_.wqkv[l, :, 0:D])
        at = put(r_.gs_qkv, l, 0, dot(r_.xeT[:, 0:R], dqb))
        put(r_.gs_qkv, l, at, r_.gkv[...].T)

        @pl.when(first)
        def _():
            dx = back_input(l)
            r_.dy[...] = dx
            below = L - 2
            sync_start(SYNCS - 1, col_sum(dx), col_sum(dx * r_.z2[below]))
            reduce_step(Q1, 0)
            s2, g2 = sync_sums(SYNCS - 1)
            r_.gshift[below, 2:3] = s2
            r_.ggain[below, 2:3] = g2

        return carry

    lax.fori_loop(0, L, backward, 0)
    for step in steps((QK0, 0), (V0, 0), (C0, 2), (E0, 5), (C1, 6), (Q1, 6), (V0, 1), (QK0, 1)):
        step()
    r_.dy[...] = back_input(0)
    in_copy = pltpu.make_async_copy(r_.dy, r_.grad_in, r_.store.at[1])
    in_copy.start()
    for step in steps(
        (C0, 3), (E0, 6), (C1, 7), (V0, 2), (QK0, 2),
        (C0, 4), (E0, 7), (C1, 8), (V0, 3), (QK0, 3),
        (C0, 5), (E0, 8), (V0, 4), (QK0, 4), (C0, 6),
    ):
        step()
    for l in range(L):
        for k in range(3):
            r_.ggain_out[k, l : l + 1] = r_.ggain[l, k : k + 1]
            r_.gshift_out[k, l : l + 1] = r_.gshift[l, k : k + 1]
    for g in range(len(GROUPS)):
        reduce_drain(g)
    sent(r_.meta.at[0 : N - 1], r_.meta_s.at[0])
    for k in range(SYNCS):
        sent(r_.st1.at[k, 0 : M * N - 1], r_.st1_s.at[k])
    for l in range(L):
        for t in range(NZ):
            sent(r_.gb.at[l, 0], r_.agp_s.at[l, t])
            if t > 0:
                sent(r_.gb.at[l, 0], r_.agc_s.at[l, t])
            if t > 1:
                sent(r_.rs1.at[l, 0], r_.rsc_s.at[l, t])
        for slot in range(2 * (NB - 1)):
            sent(r_.rs1.at[l, 0], r_.rsp_s.at[l, slot])
        for slot in range(3):
            sent(r_.ro.at[l, 0], r_.ro_s.at[l, slot])
        for side in range(2):
            sent(r_.hs.at[l, 0], r_.hal_s.at[l, side])
    act_copy.wait()
    in_copy.wait()


def finish_kernel(act_h, gin_h, *refs):
    n = len(GROUPS)
    held, (ggain_h, gshift_h), refs = refs[:n], refs[n : n + 2], refs[n + 2 :]
    act_o, gin_o, proj_o, edge_o, qkv_o, out_o, up_o, down_o, ggain_o, gshift_o = refs[:10]
    summed, refs = refs[10 : 10 + n], refs[10 + n :]
    act, gin, proj, edge, qkv, out, up, down, in_sem, out_sem = refs
    loads = [
        pltpu.make_async_copy(src, dst, in_sem.at[i])
        for i, (src, dst) in enumerate(zip(held + (act_h, gin_h), summed + (act, gin), strict=True))
    ]
    for load in loads:
        load.start()
    ggain_o[...] = ggain_h[...]
    gshift_o[...] = gshift_h[...]
    stores = []

    def store(src, dst):
        copy = pltpu.make_async_copy(src, dst, out_sem.at[len(stores)])
        copy.start()
        stores.append(copy)

    def widen(dst, l, g, at, first=0, last=None):
        rows = dst.shape[1]
        for c in range(first, dst.shape[2] // 128 if last is None else last):
            dst[l, :, 128 * c : 128 * (c + 1)] = summed[g][at : at + rows].astype(F32)
            at += rows
        return at

    for g, (name, l, first, rows, _) in enumerate(GROUPS):
        loads[g].wait()
        if name == "early":
            at = widen(out, l, g, 0)
            store(out.at[l], out_o.at[l])
            at = widen(up, l, g, at)
            store(up.at[l], up_o.at[l])
            widen(down, l, g, at)
            store(down.at[l], down_o.at[l])
        elif name == "conv":
            at = widen(proj, l, g, 0)
            store(proj.at[l], proj_o.at[l])
            widen(edge, l, g, at)
            store(edge.at[l], edge_o.at[l])
        else:
            widen(qkv, l, g, 0, first // 256, (first + rows) // 256)
            if first + rows == 1536:
                store(qkv.at[l], qkv_o.at[l])
    for i, (src, dst) in enumerate(((act, act_o), (gin, gin_o))):
        loads[n + i].wait()
        store(src, dst)
    for copy in stores:
        copy.wait()


def fused_device(
    N, M, node_input, edge_feat, graph_ids, edge_src, edge_dst, halo_send, w_proj, w_edge, w_qkv,
    w_out, w_up, w_down, norm_gain, norm_shift, cotangent,
):
    R, D = node_input.shape
    E = edge_feat.shape[0]
    L = w_proj.shape[0]
    names = scratch_list(N, M, L, R, E)
    vmem = pl.BlockSpec(memory_space=pltpu.VMEM)
    hbm = pl.BlockSpec(memory_space=pltpu.HBM)
    shape = jax.ShapeDtypeStruct
    rows = shape((R, D), F32)
    norm = shape((3, L, D), F32)
    groups = [shape((rows_g, 128), BF16) for _, _, _, rows_g, _ in GROUPS]
    outs = pl.pallas_call(
        functools.partial(kernel, N, M, L, tuple(names)),
        out_shape=[rows, rows, *groups, norm, norm],
        in_specs=[hbm] + [vmem] * 4 + [hbm] * 7 + [vmem] * 2 + [hbm],
        out_specs=[hbm] * (2 + len(GROUPS)) + [vmem] * 2,
        scratch_shapes=list(names.values()),
        compiler_params=pltpu.CompilerParams(
            collective_id=0, has_side_effects=True, vmem_limit_bytes=60 << 20
        ),
        name="layers",
    )(node_input, graph_ids, edge_src, edge_dst, halo_send, edge_feat, w_proj, w_edge, w_qkv, w_out, w_up,
      w_down, norm_gain.transpose(1, 0, 2), norm_shift.transpose(1, 0, 2), cotangent)
    weights = [shape(w.shape, F32) for w in (w_proj, w_edge, w_qkv, w_out, w_up, w_down)]
    results = pl.pallas_call(
        finish_kernel,
        out_shape=[rows, rows, *weights, norm, norm],
        in_specs=[hbm] * (2 + len(GROUPS)) + [vmem] * 2,
        out_specs=[hbm] * 8 + [vmem] * 2,
        scratch_shapes=[pltpu.VMEM(s.shape, s.dtype) for s in (*groups, rows, rows, *weights)]
        + [pltpu.SemaphoreType.DMA((len(GROUPS) + 2,)), pltpu.SemaphoreType.DMA((14,))],
        compiler_params=pltpu.CompilerParams(vmem_limit_bytes=60 << 20),
        name="gradients",
    )(*outs)
    ggain, gshift = results[8].transpose(1, 0, 2), results[9].transpose(1, 0, 2)
    return (*results[:8], ggain, gshift)


BLOCK_CAP = 2048


def extended_2(block, sides, width):
    for axis, dim in sides:
        count = lax.axis_size(axis)
        forward = [(i, i + 1) for i in range(count - 1)]
        forward.append((count - 1, 0))
        backward = [(target, source) for source, target in forward]
        low = lax.ppermute(
            lax.slice_in_dim(block, block.shape[dim] - width, None, axis=dim), axis, forward
        )
        high = lax.ppermute(lax.slice_in_dim(block, 0, width, axis=dim), axis, backward)
        block = jnp.concatenate([low, block, high], axis=dim)
    return block


def block_length(total_rows, upper_limit):
    for length in range(min(total_rows, upper_limit), 0, -1):
        if total_rows % length == 0:
            return length
    return 1


def outer_product(left, right):
    return lax.dot_general(
        left, right, (((0,), (0,)), ((), ())), preferred_element_type=jnp.float32
    )


def times_transposed(left, weight):
    return lax.dot_general(
        left, weight, (((1,), (1,)), ((), ())), preferred_element_type=jnp.float32
    )


def forward_product(left, weight):
    return jnp.dot(left, weight, preferred_element_type=jnp.float32)


def silu_slope_plain(inputs):
    logistic = jax.nn.sigmoid(inputs)
    return logistic * (1.0 + inputs * (1.0 - logistic))


def normalize(inputs, gain_row, shift_row, node_total):
    batch_mean = lax.psum(jnp.sum(inputs, 0), ("nodes", "rep")) / node_total
    centred = inputs - batch_mean
    batch_var = lax.psum(jnp.sum(centred * centred, 0), ("nodes", "rep")) / node_total
    inv_std = lax.rsqrt(batch_var + NORM_EPS)
    standard = (inputs - batch_mean) * inv_std
    return (standard * gain_row + shift_row, standard, inv_std)


def normalize_back(grad_out, standard, inv_std, gain_row, node_total):
    shift_grad, gain_grad = lax.psum(
        (jnp.sum(grad_out, 0), jnp.sum(grad_out * standard, 0)), ("nodes", "rep")
    )
    grad_in = (
        gain_row
        * inv_std
        * (grad_out - shift_grad / node_total - standard * gain_grad / node_total)
    )
    return (grad_in, gain_grad, shift_grad)


def exchange_sources(outgoing):
    halo_rows = outgoing.shape[0] // 2
    grown = extended_2(outgoing, (("nodes", 0),), halo_rows)
    return jnp.concatenate([grown[:halo_rows], grown[3 * halo_rows :]], 0)


def return_sources(incoming_grad):
    halo_rows = incoming_grad.shape[0] // 2
    grown = extended_2(incoming_grad.astype(jnp.bfloat16), (("nodes", 0),), halo_rows).astype(
        incoming_grad.dtype
    )
    return jnp.concatenate([grown[:halo_rows], grown[3 * halo_rows :]], 0)


def attend_forward(query_rows, key_rows, value_rows, local_graphs, group_graphs):
    row_count = query_rows.shape[0]
    score_scale = HEAD_DIM ** (-0.5)
    queries = query_rows.reshape(row_count, HEADS, HEAD_DIM)

    def add_piece(carried, kv_piece, first_row):
        key_piece, value_piece = kv_piece
        piece_rows = key_piece.shape[0]
        block_len = block_length(piece_rows, BLOCK_CAP)

        def add_block(block_state, block_index):
            row_max, row_sum, accumulated = block_state
            block_start = block_index * block_len
            key_block = lax.dynamic_slice_in_dim(key_piece, block_start, block_len, 0).reshape(
                block_len, HEADS, HEAD_DIM
            )
            value_block = lax.dynamic_slice_in_dim(value_piece, block_start, block_len, 0).reshape(
                block_len, HEADS, HEAD_DIM
            )
            key_graphs = lax.dynamic_slice_in_dim(
                group_graphs, first_row + block_start, block_len, 0
            )
            same_graph = (local_graphs[:, None] == key_graphs[None, :])[None]
            scores = (
                jnp.einsum("qhd,khd->hqk", queries, key_block, preferred_element_type=jnp.float32)
                * score_scale
            )
            scores = jnp.where(same_graph, scores, NEG)
            new_max = jnp.maximum(row_max, jnp.max(scores, 2))
            weights = jnp.where(same_graph, jnp.exp(scores - new_max[:, :, None]), 0.0)
            factor = jnp.exp(row_max - new_max)
            row_sum = row_sum * factor + jnp.sum(weights, 2)
            contrib = jnp.einsum(
                "hqk,khd->qhd",
                weights.astype(jnp.bfloat16),
                value_block,
                preferred_element_type=jnp.float32,
            )
            accumulated = accumulated * jnp.transpose(factor)[:, :, None] + contrib
            return ((new_max, row_sum, accumulated), None)

        carried, _ = lax.scan(add_block, carried, jnp.arange(piece_rows // block_len))
        return carried

    start_state = (
        jnp.full((HEADS, row_count), NEG, jnp.float32),
        jnp.zeros((HEADS, row_count), jnp.float32),
        jnp.zeros((row_count, HEADS, HEAD_DIM), jnp.float32),
    )
    row_max, row_sum, accumulated = add_piece(
        start_state,
        (
            lax.all_gather(key_rows, "nodes", axis=0, tiled=True),
            lax.all_gather(value_rows, "nodes", axis=0, tiled=True),
        ),
        jnp.int32(0),
    )
    attn_raw = accumulated / jnp.transpose(row_sum)[:, :, None]
    log_sum = row_max + jnp.log(row_sum)
    return (attn_raw, log_sum)


def attend_backward(
    query_rows, key_rows, value_rows, grad_low, attn_raw, log_sum, local_graphs, group_graphs
):
    row_count = query_rows.shape[0]
    model_width = HEADS * HEAD_DIM
    score_scale = HEAD_DIM ** (-0.5)
    queries = query_rows.reshape(row_count, HEADS, HEAD_DIM)
    grad_heads = grad_low.reshape(row_count, HEADS, HEAD_DIM)
    row_delta = jnp.einsum("qhd,qhd->hq", grad_heads.astype(jnp.float32), attn_raw)

    def score_block(key_block, value_block, key_graphs):
        same_graph = (local_graphs[:, None] == key_graphs[None, :])[None]
        scores = (
            jnp.einsum("qhd,khd->hqk", queries, key_block, preferred_element_type=jnp.float32)
            * score_scale
        )
        attn_weights = jnp.exp(jnp.where(same_graph, scores - log_sum[:, :, None], NEG))
        grad_weights = jnp.einsum(
            "qhd,khd->hqk", grad_heads, value_block, preferred_element_type=jnp.float32
        )
        grad_scores = (attn_weights * (grad_weights - row_delta[:, :, None])).astype(jnp.bfloat16)
        return (attn_weights, grad_scores)

    def key_terms(attn_weights, grad_scores, block_len):
        grad_keys = (
            jnp.einsum("hqk,qhd->khd", grad_scores, queries, preferred_element_type=jnp.float32)
            * score_scale
        )
        grad_values = jnp.einsum(
            "hqk,qhd->khd",
            attn_weights.astype(jnp.bfloat16),
            grad_heads,
            preferred_element_type=jnp.float32,
        )
        return jnp.concatenate(
            [
                grad_keys.reshape(block_len, model_width),
                grad_values.reshape(block_len, model_width),
            ],
            1,
        )

    def query_term(grad_scores, key_block):
        return (
            jnp.einsum("hqk,khd->qhd", grad_scores, key_block, preferred_element_type=jnp.float32)
            * score_scale
        )

    group_rows = group_graphs.shape[0]

    def add_piece(carried, kv_piece, first_row):
        key_piece, value_piece = kv_piece
        piece_rows = key_piece.shape[0]
        block_len = block_length(piece_rows, BLOCK_CAP)

        def add_block(block_state, block_index):
            grad_query, buffer = block_state
            block_start = block_index * block_len
            key_block = lax.dynamic_slice_in_dim(key_piece, block_start, block_len, 0).reshape(
                block_len, HEADS, HEAD_DIM
            )
            value_block = lax.dynamic_slice_in_dim(value_piece, block_start, block_len, 0).reshape(
                block_len, HEADS, HEAD_DIM
            )
            place = first_row + block_start
            key_graphs = lax.dynamic_slice_in_dim(group_graphs, place, block_len, 0)
            attn_weights, grad_scores = score_block(key_block, value_block, key_graphs)
            grad_query = grad_query + query_term(grad_scores, key_block)
            block_terms = key_terms(attn_weights, grad_scores, block_len)
            current = lax.dynamic_slice_in_dim(buffer, place, block_len, 0)
            buffer = lax.dynamic_update_slice_in_dim(buffer, current + block_terms, place, 0)
            return ((grad_query, buffer), None)

        carried, _ = lax.scan(add_block, carried, jnp.arange(piece_rows // block_len))
        return carried

    start_state = (
        jnp.zeros((row_count, HEADS, HEAD_DIM), jnp.float32),
        jnp.zeros((group_rows, 2 * model_width), jnp.float32),
    )
    grad_query, buffer = add_piece(
        start_state,
        (
            lax.all_gather(key_rows, "nodes", axis=0, tiled=True),
            lax.all_gather(value_rows, "nodes", axis=0, tiled=True),
        ),
        jnp.int32(0),
    )
    grad_kv = lax.psum_scatter(buffer, "nodes", scatter_dimension=0, tiled=True)
    return (
        grad_query.reshape(row_count, model_width),
        grad_kv[:, :model_width],
        grad_kv[:, model_width:],
    )


def layer_forward(
    hidden, params, edge_feat, edge_src, edge_dst, halo_send, local_graphs, group_graphs, node_total
):
    w_proj, w_edge, w_qkv, w_out, w_up, w_down, norm_gains, norm_shifts = params
    row_count, model_width = hidden.shape
    hidden_low = hidden.astype(jnp.bfloat16)
    projected = forward_product(hidden_low, w_proj)
    self_term = projected[:, :model_width]
    dest_term = projected[:, 2 * model_width : 3 * model_width]
    source_rows = jnp.concatenate(
        [projected[:, model_width : 2 * model_width], projected[:, 3 * model_width :]], 1
    ).astype(jnp.bfloat16)
    incoming = exchange_sources(source_rows[halo_send])
    extended = jnp.concatenate([source_rows, incoming], 0)
    edge_rows = extended[edge_src].astype(jnp.float32)
    source_b = edge_rows[:, :model_width]
    source_e = edge_rows[:, model_width:]
    edge_proj = forward_product(edge_feat, w_edge)
    gating = jax.nn.sigmoid(dest_term[edge_dst] + source_e + edge_proj)
    numerator = jax.ops.segment_sum(gating * source_b, edge_dst, row_count)
    denominator = jax.ops.segment_sum(gating, edge_dst, row_count)
    message = self_term + numerator / (denominator + GATE_EPS)
    normed_one, standard_one, inv_one = normalize(
        message, norm_gains[0], norm_shifts[0], node_total
    )
    local_out = hidden + jax.nn.silu(normed_one)
    qkv_low = forward_product(hidden_low, w_qkv).astype(jnp.bfloat16)
    query_rows = qkv_low[:, :model_width]
    key_rows = qkv_low[:, model_width : 2 * model_width]
    value_rows = qkv_low[:, 2 * model_width :]
    attn_raw, log_sum = attend_forward(query_rows, key_rows, value_rows, local_graphs, group_graphs)
    attn_low = attn_raw.reshape(row_count, model_width).astype(jnp.bfloat16)
    attn_proj = forward_product(attn_low, w_out)
    normed_two, standard_two, inv_two = normalize(
        hidden + attn_proj, norm_gains[1], norm_shifts[1], node_total
    )
    mixed = local_out + normed_two
    mixed_low = mixed.astype(jnp.bfloat16)
    up_proj = forward_product(mixed_low, w_up)
    activated = jax.nn.silu(up_proj).astype(jnp.bfloat16)
    down_proj = forward_product(activated, w_down)
    normed_three, standard_three, inv_three = normalize(
        mixed + down_proj, norm_gains[2], norm_shifts[2], node_total
    )
    saved = (
        hidden_low,
        source_b,
        gating,
        numerator,
        denominator,
        normed_one,
        standard_one,
        inv_one,
        query_rows,
        key_rows,
        value_rows,
        attn_raw,
        log_sum,
        attn_low,
        standard_two,
        inv_two,
        mixed_low,
        up_proj,
        activated,
        standard_three,
        inv_three,
    )
    return (normed_three, saved)


def layer_backward(
    grad_out,
    params,
    saved,
    edge_feat,
    edge_src,
    edge_dst,
    halo_send,
    local_graphs,
    group_graphs,
    node_total,
):
    w_proj, w_edge, w_qkv, w_out, w_up, w_down, norm_gains, norm_shifts = params
    (
        hidden_low,
        source_b,
        gating,
        numerator,
        denominator,
        normed_one,
        standard_one,
        inv_one,
        query_rows,
        key_rows,
        value_rows,
        attn_raw,
        log_sum,
        attn_low,
        standard_two,
        inv_two,
        mixed_low,
        up_proj,
        activated,
        standard_three,
        inv_three,
    ) = saved
    row_count, model_width = grad_out.shape
    grad_three, gain_three, shift_three = normalize_back(
        grad_out, standard_three, inv_three, norm_gains[2], node_total
    )
    down_grad = grad_three.astype(jnp.bfloat16)
    grad_w_down = outer_product(activated, down_grad)
    up_grad = (times_transposed(down_grad, w_down) * silu_slope_plain(up_proj)).astype(jnp.bfloat16)
    grad_w_up = outer_product(mixed_low, up_grad)
    grad_mixed = grad_three + times_transposed(up_grad, w_up)
    grad_two, gain_two, shift_two = normalize_back(
        grad_mixed, standard_two, inv_two, norm_gains[1], node_total
    )
    out_grad = grad_two.astype(jnp.bfloat16)
    grad_w_out = outer_product(attn_low, out_grad)
    attn_grad = times_transposed(out_grad, w_out).astype(jnp.bfloat16)
    grad_query, grad_key, grad_value = attend_backward(
        query_rows, key_rows, value_rows, attn_grad, attn_raw, log_sum, local_graphs, group_graphs
    )
    qkv_grad = jnp.concatenate([grad_query, grad_key, grad_value], 1).astype(jnp.bfloat16)
    grad_w_qkv = outer_product(hidden_low, qkv_grad)
    grad_message, gain_one, shift_one = normalize_back(
        grad_mixed * silu_slope_plain(normed_one), standard_one, inv_one, norm_gains[0], node_total
    )
    shifted = denominator + GATE_EPS
    grad_numer = grad_message / shifted
    grad_denom = -grad_message * numerator / (shifted * shifted)
    numer_edge = grad_numer[edge_dst]
    grad_gate = numer_edge * source_b + grad_denom[edge_dst]
    grad_pre_edge = grad_gate * gating * (1.0 - gating)
    edge_grad = grad_pre_edge.astype(jnp.bfloat16)
    grad_w_edge = outer_product(edge_feat, edge_grad)
    grad_dest = jax.ops.segment_sum(grad_pre_edge, edge_dst, row_count)
    grad_extended = jax.ops.segment_sum(
        jnp.concatenate([numer_edge * gating, grad_pre_edge], 1),
        edge_src,
        row_count + halo_send.shape[0],
    )
    returned = return_sources(grad_extended[row_count:])
    grad_source = grad_extended[:row_count].at[halo_send].add(returned)
    proj_grad = jnp.concatenate(
        [grad_message, grad_source[:, :model_width], grad_dest, grad_source[:, model_width:]], 1
    ).astype(jnp.bfloat16)
    grad_w_proj = outer_product(hidden_low, proj_grad)
    grad_hidden = (
        grad_mixed
        + grad_two
        + times_transposed(proj_grad, w_proj)
        + times_transposed(qkv_grad, w_qkv)
    )
    weight_grads = (grad_w_proj, grad_w_edge, grad_w_qkv, grad_w_out, grad_w_up, grad_w_down)
    return (
        grad_hidden,
        weight_grads,
        jnp.stack([gain_one, gain_two, gain_three]),
        jnp.stack([shift_one, shift_two, shift_three]),
    )


def per_device(
    node_input,
    edge_feat,
    graph_ids,
    edge_src,
    edge_dst,
    halo_send,
    w_proj,
    w_edge,
    w_qkv,
    w_out,
    w_up,
    w_down,
    norm_gain,
    norm_shift,
    cotangent,
):
    group_graphs = lax.all_gather(graph_ids, "nodes", axis=0, tiled=True)
    node_total = node_input.shape[0] * lax.axis_size("nodes") * lax.axis_size("rep")
    layer_count = w_proj.shape[0]
    layer_params = [
        (
            w_proj[layer_index],
            w_edge[layer_index],
            w_qkv[layer_index],
            w_out[layer_index],
            w_up[layer_index],
            w_down[layer_index],
            norm_gain[layer_index],
            norm_shift[layer_index],
        )
        for layer_index in range(layer_count)
    ]
    hidden = node_input.astype(jnp.float32)
    saved_all = []
    for layer_index in range(layer_count):
        hidden, saved = layer_forward(
            hidden,
            layer_params[layer_index],
            edge_feat,
            edge_src,
            edge_dst,
            halo_send,
            graph_ids,
            group_graphs,
            node_total,
        )
        saved_all.append(saved)
    grad_hidden = cotangent.astype(jnp.float32)
    weight_parts = [None] * layer_count
    gain_parts = [None] * layer_count
    shift_parts = [None] * layer_count
    for layer_index in range(layer_count - 1, -1, -1):
        (
            grad_hidden,
            weight_parts[layer_index],
            gain_parts[layer_index],
            shift_parts[layer_index],
        ) = layer_backward(
            grad_hidden,
            layer_params[layer_index],
            saved_all[layer_index],
            edge_feat,
            edge_src,
            edge_dst,
            halo_send,
            graph_ids,
            group_graphs,
            node_total,
        )
    proj_local = jnp.stack([weight_parts[layer_index][0] for layer_index in range(layer_count)])
    edge_local = jnp.stack([weight_parts[layer_index][1] for layer_index in range(layer_count)])
    qkv_local = jnp.stack([weight_parts[layer_index][2] for layer_index in range(layer_count)])
    out_local = jnp.stack([weight_parts[layer_index][3] for layer_index in range(layer_count)])
    up_local = jnp.stack([weight_parts[layer_index][4] for layer_index in range(layer_count)])
    down_local = jnp.stack([weight_parts[layer_index][5] for layer_index in range(layer_count)])
    grad_proj, grad_edge, grad_qkv, grad_out, grad_up, grad_down = lax.psum(
        (proj_local, edge_local, qkv_local, out_local, up_local, down_local), ("nodes", "rep")
    )
    return (
        hidden,
        grad_hidden,
        grad_proj,
        grad_edge,
        grad_qkv,
        grad_out,
        grad_up,
        grad_down,
        jnp.stack(gain_parts),
        jnp.stack(shift_parts),
    )


def solution(mesh):
    in_specs = (
        P(("rep", "nodes"), None),
        P(("rep", "nodes"), None),
        P(("rep", "nodes")),
        P(("rep", "nodes")),
        P(("rep", "nodes")),
        P(("rep", "nodes")),
        P(),
        P(),
        P(),
        P(),
        P(),
        P(),
        P(),
        P(),
        P(("rep", "nodes"), None),
    )
    out_specs = (
        P(("rep", "nodes"), None),
        P(("rep", "nodes"), None),
        P(),
        P(),
        P(),
        P(),
        P(),
        P(),
        P(),
        P(),
    )
    N, M = mesh.shape["nodes"], mesh.shape["rep"]
    fused = N in (4, 8) and M % 2 == 0 and 512 % (16 * N * M) == 0
    return jax.shard_map(
        functools.partial(fused_device, N, M) if fused else per_device,
        mesh=mesh, in_specs=in_specs, out_specs=out_specs, check_vma=False,
    )
```

```python
import functools
import math

import jax
import jax.numpy as jnp
from jax import lax
from jax.experimental import pallas as pl
from jax.experimental.pallas import tpu as pltpu
from jax.sharding import PartitionSpec as P

HEADS = 8
HEAD_DIM = 32
NEG = -1e30
NORM_EPS = 1e-05
GATE_EPS = 1e-06
F32, BF16, I32 = jnp.float32, jnp.bfloat16, jnp.int32
MESH = pl.DeviceIdType.MESH
SYNCS = 12
STRIP = 32
GROUPS = (
    ("early", 1, 0, 2560, ("core", "y", "nodes")),
    ("conv", 1, 0, 2560, ("core", "x", "y", "z")),
    ("qkv", 1, 0, 1536, ("core", "y", "nodes")),
    ("early", 0, 0, 2560, ("core", "x", "y", "z")),
    ("conv", 0, 0, 2560, ("core", "y", "nodes")),
    ("qkv", 0, 0, 1024, ("rep", "nodes")),
    ("qkv", 0, 1024, 512, ("nodes", "rep")),
)


def dot(left, right):
    return lax.dot_general(
        left, right, (((1,), (0,)), ((), ())), preferred_element_type=F32
    )


def dot_nt(left, right):
    return lax.dot_general(
        left, right, (((1,), (1,)), ((), ())), preferred_element_type=F32
    )


def dot_tn(left, right):
    return lax.dot_general(
        left, right, (((0,), (0,)), ((), ())), preferred_element_type=F32
    )


def split(value):
    high = value.astype(BF16)
    return high, (value - high.astype(F32)).astype(BF16)


def sigmoid(value):
    return jax.nn.sigmoid(value)


def silu_slope(value):
    logistic = sigmoid(value)
    return logistic * (1.0 + value * (1.0 - logistic))


def col_sum(value):
    return jnp.sum(value, axis=0, keepdims=True)


def pack(first, second):
    return jnp.concatenate([first[:, :128], first[:, 128:], second[:, :128], second[:, 128:]], 0)


def unpack(tile):
    return [jnp.concatenate([tile[i : i + 1], tile[i + 1 : i + 2]], 1) for i in (0, 2)]


def combine_moments(tiles, count):
    mean = jnp.mean(tiles[:, 0:2], 0)
    off = tiles[:, 0:2] - mean
    return jnp.concatenate([mean, jnp.sum(tiles[:, 2:4] + count * off * off, 0)], 0)


class Refs:
    pass


def axis_sizes(N, M):
    return dict(core=2, y=M // 2, x=2, z=N // 2, rep=M, nodes=N)


def scratch_list(N, M, L, R, E):
    NZ, NB, G = N // 2, N // 4, N * R
    D, FF, W, HH = 256, 512, 4 * R, HEADS // 2 * R
    dma = lambda *shape: pltpu.SemaphoreType.DMA(shape)
    vm = lambda dtype, *shape: pltpu.VMEM(shape, dtype)
    names = dict(
        gb=vm(BF16, L, N, R, D),
        xs=vm(BF16, L, N, R, D),
        meta=vm(I32, N, 8, 256),
        cot=vm(BF16, R, D),
        wp=vm(BF16, L, D, 4 * D),
        we=vm(BF16, L, D, D),
        wqkv=vm(BF16, L, D, 3 * D),
        wo=vm(BF16, L, D, D),
        wu=vm(BF16, L, D, FF),
        wd=vm(BF16, L, FF, D),
        st1=vm(F32, SYNCS, M * N, 4, 128),
        gain=vm(F32, L, 8, D),
        shift=vm(F32, L, 8, D),
        ggain=vm(F32, L, 8, D),
        gshift=vm(F32, L, 8, D),
        iv=vm(F32, L, 8, D),
        moff=vm(F32, N, 8, D),
        move=vm(F32, 8, D),
        le=vm(BF16, E, 1024),
        re=vm(BF16, 1024, D),
        TT=vm(BF16, R, 2 * E),
        ST=vm(BF16, 256, E),
        efT=vm(BF16, D, E),
        HP=vm(BF16, 32, R),
        HN=vm(BF16, 32, R),
        A=vm(BF16, R, 64),
        bias=vm(F32, R, G),
        xf=vm(F32, L + 1, R, D),
        xe=vm(BF16, L, 256, D),
        xeT=vm(BF16, D, 256),
        gate=vm(F32, L, E, D),
        bs=vm(BF16, L, E, D),
        num=vm(F32, L, R, D),
        den=vm(F32, L, R, D),
        z0=vm(F32, L, R, D),
        z1=vm(F32, L, R, D),
        z2=vm(F32, L, R, D),
        wkvT=vm(BF16, L, 2 * D, D),
        kvT=vm(BF16, L, 2 * D, G),
        odT=vm(F32, NB, D, R),
        ldT=vm(F32, NB, D, R),
        md=vm(F32, NB, R, D),
        rb=vm(F32, L, NB, R, D),
        pst=vm(BF16, L, HEADS * R, G),
        oraw=vm(F32, L, R, D),
        ob=vm(BF16, L, R, D),
        mb=vm(BF16, L, R, D),
        u=vm(F32, L, R, FF),
        g=vm(BF16, L, R, FF),
        dy=vm(F32, R, D),
        dmix=vm(F32, R, D),
        gy0=vm(F32, R, D),
        local=vm(F32, R, D),
        dxo=vm(F32, R, D),
        dob=vm(F32, R, D),
        dqT=vm(F32, D, R),
        qm=vm(BF16, L, 2, HH, 128),
        q=vm(BF16, L, R, D),
        qT=vm(BF16, D, R),
        dosT=vm(BF16, 128, R),
        dom=vm(BF16, HH, 256),
        sc=vm(F32, 2, max(2 * R, E), W),
        tp=vm(F32, HEADS // 2, R, 128),
        dss=vm(BF16, HH, W),
        dkv=vm(BF16, 2 * D, W),
        gkv=vm(F32, 2 * D, D),
        gg=vm(BF16, 2 * E, 2 * D),
        dn=vm(BF16, 512, 2 * D),
        dproj=vm(BF16, 256, 4 * D),
        dxs=vm(BF16, L, NZ, 2, R, D),
        rs1=vm(BF16, L, NZ, R, D),
        cs=vm(BF16, L, NZ, R, D),
        rs2=vm(BF16, L, NZ, R, D),
        ro=vm(BF16, L, 3, R, D),
        hs=vm(BF16, L, 2, 32, D),
        hr=vm(BF16, L, 2, 32, D),
    )
    names.update(
        gs_early=vm(BF16, L, 2560, 128),
        gs_conv=vm(BF16, L, 2560, 128),
        gs_qkv=vm(BF16, L, 1536, 128),
    )
    sizes = axis_sizes(N, M)
    for g, (_, _, _, rows, stages) in enumerate(GROUPS):
        names[f"go{g}"] = vm(BF16, rows, 128)
        left = rows
        for k, axis in enumerate(stages):
            left //= sizes[axis]
            names[f"ga{g}_{k}"] = vm(BF16, sizes[axis] - 1, left, 128)
            if k < len(stages) - 1:
                names[f"gh{g}_{k}"] = vm(BF16, left, 128)
    names.update(
        ar_s=dma(len(GROUPS)),
        ar_r=dma(sum(2 * len(stages) for *_, stages in GROUPS)),
        ar_l=dma(len(GROUPS)),
        load=dma(9),
        store=dma(2),
        meta_s=dma(1),
        meta_r=dma(1),
        st_s=dma(1),
        st_r=dma(SYNCS),
        ag_s=dma(1),
        agn_r=dma(L),
        agc_r=dma(L, NZ),
        agp_r=dma(L),
        rs_s=dma(1),
        rsp_r=dma(L, NB),
        ro_r=dma(L),
        rsc_r=dma(L),
        hal_s=dma(1),
        hal_r=dma(L),
    )
    return names


IN_NAMES = (
    "x_in", "ids", "edge_src", "edge_dst", "halo", "ef_h", "wp_h", "we_h", "wqkv_h", "wo_h", "wu_h", "wd_h",
    "gain_in", "shift_in", "cot_h",
)
OUT_NAMES = ("out_act", "grad_in", *(f"gout{g}" for g in range(len(GROUPS))), "ggain_out", "gshift_out")


def kernel(N, M, L, names, *args):
    r_ = Refs()
    for name, ref in zip(IN_NAMES + OUT_NAMES + tuple(names), args, strict=True):
        setattr(r_, name, ref)
    R, D = r_.x_in.shape
    E = r_.ef_h.shape[0]
    NZ, NB, G, W = N // 2, N // 4, N * R, 4 * R
    HK = HEADS // 2
    total = float(N * M * R)
    scale = HEAD_DIM ** -0.5
    me = lax.axis_index("nodes")
    rep = lax.axis_index("rep")
    z = me // 2
    par = me % 2
    partner = 2 * z + (1 - par)
    prev = (me + N - 1) % N
    nxt = (me + 1) % N
    zh, zl = z // 2, z % 2
    z_to = lambda t: 2 * ((zh + t // 2) % NB) + (zl + t % 2) % 2
    z_from = lambda t: 2 * ((zh + NB - t // 2) % NB) + (zl + t % 2) % 2

    def remote(src, dst, s_sem, r_sem, **where):
        return pltpu.make_async_remote_copy(
            src_ref=src, dst_ref=dst, send_sem=s_sem, recv_sem=r_sem,
            device_id=where, device_id_type=MESH,
        )

    def send(src, dst, s_sem, r_sem, **where):
        remote(src, dst, s_sem, r_sem, **where).start()

    def send_rows(src, dst, rows, s_sem, r_sem, **where):
        pieces = next(p for p in range(1, rows) if rows % (16 * p) == 0 and rows // p <= 128)
        for at in range(0, rows, rows // pieces):
            cut = pl.ds(at, rows // pieces)
            send(src.at[cut], dst.at[cut], s_sem, r_sem, **where)

    def arrive(dst, r_sem):
        remote(dst, dst, r_sem, r_sem, nodes=partner).wait_recv()

    def sent(src, s_sem):
        remote(src, src, s_sem, s_sem, nodes=partner).wait_send()

    def when(condition, *acts):
        @pl.when(condition)
        def _():
            for act in acts:
                act()

    loads = [pltpu.make_async_copy(r_.ef_h, r_.le.at[:, D : 2 * D], r_.load.at[0])] + [
        pltpu.make_async_copy(getattr(r_, f"{name}_h"), getattr(r_, name), r_.load.at[1 + i])
        for i, name in enumerate(("we", "wqkv", "wp", "wo", "wu", "wd", "cot"))
    ]
    own_rows = pltpu.make_async_copy(r_.x_in, r_.gb.at[0, me], r_.load.at[8])
    own_rows.start()
    for load in loads:
        load.start()

    barrier = pltpu.get_barrier_semaphore()
    for dr in range(M):
        for d in range(N):
            if dr + d > 0:
                pl.semaphore_signal(barrier, inc=1, device_id={"rep": (rep + dr) % M, "nodes": (me + d) % N},
                                    device_id_type=MESH)
    pl.semaphore_wait(barrier, M * N - 1)

    def gather_start(l):
        mine = r_.gb.at[l, me]
        send_rows(mine, mine, R, r_.ag_s.at[0], r_.agn_r.at[l], nodes=partner)
        send_rows(mine, mine, R, r_.ag_s.at[0], r_.agn_r.at[l], nodes=2 * z_to(1) + par)
        send_rows(mine, mine, R, r_.ag_s.at[0], r_.agn_r.at[l], nodes=2 * z_to(1) + 1 - par)
        for t in range(2, NZ):
            send_rows(mine, mine, R, r_.ag_s.at[0], r_.agc_r.at[l, t], nodes=2 * z_to(t) + par)

    def gather_pass(l, t):
        piece = r_.gb.at[l, 2 * z_from(t) + par]
        arrive(piece, r_.agc_r.at[l, t])
        send_rows(piece, piece, R, r_.ag_s.at[0], r_.agp_r.at[l], nodes=partner)

    def gather_near(l):
        arrive(r_.gb.at[l, 0:3], r_.agn_r.at[l])

    def gather_far(l):
        arrive(r_.gb.at[l, 0 : NZ - 2], r_.agp_r.at[l])

    def sync_start(k, first, second):
        mine = rep * N + me
        r_.st1[k, mine] = pack(first, second)
        for dr in range(M):
            for d in range(N):
                if dr + d > 0:
                    send(r_.st1.at[k, mine], r_.st1.at[k, mine], r_.st_s.at[0], r_.st_r.at[k],
                         rep=(rep + dr) % M, nodes=(me + d) % N)

    def sync_wait(k):
        arrive(r_.st1.at[k, 0 : M * N - 1], r_.st_r.at[k])

    def sync_moments(k):
        sync_wait(k)
        return unpack(combine_moments(r_.st1[k], float(R)))

    def sync_sums(k):
        sync_wait(k)
        return unpack(jnp.sum(r_.st1[k], 0))

    sizes = axis_sizes(N, M)
    core, row = rep % 2, rep // 2
    places = dict(
        core=(core, lambda t: dict(rep=2 * row + t)),
        y=(row, lambda t: dict(rep=2 * t + core)),
        x=(par, lambda t: dict(nodes=2 * z + t)),
        z=(z, lambda t: dict(nodes=2 * t + par)),
        rep=(rep, lambda t: dict(rep=t)),
        nodes=(me, lambda t: dict(nodes=t)),
    )

    def reduce_step(g, step):
        name, layer, first, rows, stages = GROUPS[g]
        K = len(stages)
        base = sum(2 * len(before) for *_, before in GROUPS[:g])
        gs, out = getattr(r_, f"gs_{name}").at[layer, first : first + rows], getattr(r_, f"go{g}")
        count, offset = [rows], [0]
        for axis in stages:
            count.append(count[-1] // sizes[axis])
            offset.append(offset[-1] + places[axis][0] * count[-1])
        take = lambda start, size: pl.ds(pl.multiple_of(start, 16), size)
        if 1 <= step <= K:
            k = step - 1
            got = getattr(r_, f"ga{g}_{k}")
            arrive(got, r_.ar_r.at[base + k])
            held = gs if k == 0 else getattr(r_, f"gh{g}_{k - 1}")
            index = places[stages[k]][0]
            acc = held[take(index * count[k + 1], count[k + 1])].astype(F32)
            for slot in range(sizes[stages[k]] - 1):
                acc = acc + got[slot].astype(F32)
            if step < K:
                getattr(r_, f"gh{g}_{k}")[...] = acc.astype(BF16)
            else:
                out[take(offset[K], count[K])] = acc.astype(BF16)
        elif step > K:
            k = 2 * K - step
            arrive(out.at[0 : (sizes[stages[k]] - 1) * count[k + 1]], r_.ar_r.at[base + step - 1])
        if step < K:
            held = gs if step == 0 else getattr(r_, f"gh{g}_{step - 1}")
            index, device = places[stages[step]]
            size = sizes[stages[step]]
            for d in range(1, size):
                to = (index + d) % size
                send_rows(held.at[take(to * count[step + 1], count[step + 1])], getattr(r_, f"ga{g}_{step}").at[d - 1],
                     count[step + 1], r_.ar_s.at[g], r_.ar_r.at[base + step], **device(to))
        elif step < 2 * K:
            k = 2 * K - 1 - step
            index, device = places[stages[k]]
            size = sizes[stages[k]]
            here = out.at[take(offset[k + 1], count[k + 1])]
            for d in range(1, size):
                send_rows(here, here, count[k + 1], r_.ar_s.at[g], r_.ar_r.at[base + step],
                          **device((index + d) % size))
        else:
            pltpu.make_async_copy(out, getattr(r_, f"gout{g}"), r_.ar_l.at[g]).start()

    def reduce_drain(g):
        name, _, _, rows, _ = GROUPS[g]
        sent(getattr(r_, f"gs_{name}").at[:, 0 : rows - rows // (M * N)], r_.ar_s.at[g])
        pltpu.make_async_copy(getattr(r_, f"go{g}"), getattr(r_, f"gout{g}"), r_.ar_l.at[g]).wait()

    def put(buf, l, at, value):
        rows = value.shape[0]
        for c in range(value.shape[1] // 128):
            buf[l, at : at + rows] = value[:, 128 * c : 128 * (c + 1)].astype(BF16)
            at += rows
        return at

    lane_head = lax.broadcasted_iota(I32, (R, 128), 1) // HEAD_DIM

    def by_head(parts):
        out = parts[0]
        for k in range(1, HK):
            out = jnp.where(lane_head == k, parts[k], out)
        return out

    r_.meta[me] = jnp.full((8, 256), -1, I32)
    r_.meta[me, 0:1, 0:R] = r_.ids[...].reshape(1, R)
    r_.meta[me, 1:2, 0:48] = r_.halo[...].reshape(1, 48)
    for d in range(1, N):
        send(r_.meta.at[me], r_.meta.at[me], r_.meta_s.at[0], r_.meta_r.at[0], nodes=(me + d) % N)
    own_rows.wait()
    gather_start(0)

    src_row = r_.edge_src[...].reshape(1, E)
    src_row = jnp.where(src_row < R + 24, src_row, src_row + 8)
    dst_row = r_.edge_dst[...].reshape(1, E)
    src_col = jnp.broadcast_to(src_row, (128, E)).T[:, 0:1]
    dst_col = jnp.broadcast_to(dst_row, (128, E)).T[:, 0:1]
    as_mask = lambda cond: cond.astype(F32).astype(BF16)
    r_.le[:, 0:256] = as_mask(src_col == lax.broadcasted_iota(I32, (E, 256), 1))
    target = as_mask(dst_col == lax.broadcasted_iota(I32, (E, 256), 1))
    r_.le[:, 512:768] = target
    r_.le[:, 768:1024] = target
    target = as_mask(dst_row == lax.broadcasted_iota(I32, (R, E), 0))
    r_.TT[:, 0:E] = target
    r_.TT[:, E:] = target
    r_.ST[...] = as_mask(src_row == lax.broadcasted_iota(I32, (256, E), 0))
    r_.dn[R:256] = jnp.zeros((256 - R, 2 * D), BF16)
    r_.dn[256 + R : 512] = jnp.zeros((256 - R, 2 * D), BF16)
    r_.dproj[R:256, 0:D] = jnp.zeros((256 - R, D), BF16)
    r_.dproj[R:256, 2 * D : 3 * D] = jnp.zeros((256 - R, D), BF16)
    loads[0].wait()
    r_.efT[...] = r_.le[:, D : 2 * D].T
    for l in range(L):
        for k in range(3):
            r_.gain[l, k : k + 1] = r_.gain_in[k, l : l + 1]
            r_.shift[l, k : k + 1] = r_.shift_in[k, l : l + 1]
    r_.xf[0] = r_.gb[0, me].astype(F32)
    r_.moff[...] = jnp.zeros((N, 8, D), F32)
    r_.move[0:1] = jnp.ones((1, D), F32)
    r_.move[1:2] = jnp.zeros((1, D), F32)
    for load in loads[1:]:
        load.wait()
    for l in range(L):
        r_.wkvT[l] = r_.wqkv[l, :, D:].T

    arrive(r_.meta.at[0 : N - 1], r_.meta_r.at[0])
    id_col = jnp.broadcast_to(r_.meta[me][0:1, 0:R], (128, R)).T[:, 0:1]
    id_row = jnp.concatenate([r_.meta[j][0:1, 0:R] for j in range(N)], 1)
    r_.bias[...] = jnp.where(id_col == id_row, 0.0, NEG)

    def halo_onehot(device, start):
        col = jnp.broadcast_to(r_.meta[device][1:2, 0:128], (128, 128)).T[start : start + 24, 0:1]
        hot = (col == lax.broadcasted_iota(I32, (24, R), 1)).astype(F32)
        return jnp.concatenate([hot, jnp.zeros((8, R), F32)], 0).astype(BF16)

    r_.HP[...] = halo_onehot(prev, 24)
    r_.HN[...] = halo_onehot(nxt, 0)
    r_.A[...] = as_mask(r_.meta[me][1:2, 0:64] == lax.broadcasted_iota(I32, (R, 64), 0))

    factor_exp = scale * math.log2(math.e)

    def prepare_queries(l):
        q = dot(r_.xs[l, me], r_.wqkv[l, :, :D]).astype(BF16)
        r_.q[l] = q
        q = q.astype(F32)
        for hf in range(2):
            for k in range(HK):
                part = jnp.where(lane_head == k, q[:, 128 * hf : 128 * (hf + 1)], 0.0)
                r_.qm[l, hf, k * R : (k + 1) * R] = part.astype(BF16)

    def head_dims(hf, k, base=0):
        return pl.ds(pl.multiple_of(base + hf * 128 + k * HEAD_DIM, HEAD_DIM), HEAD_DIM)

    def head_rows(hf, k, count=1):
        return pl.ds(pl.multiple_of((hf * HK + k) * R, 64), count * R)

    def lane_half(hf):
        return pl.ds(pl.multiple_of(hf * 128, 128), 128)

    def half_of(i):
        half = (zh + NB - i) % NB
        return half, pl.ds(pl.multiple_of(half * W, 128), W)

    def attention_keys(l, i):
        half, rows = half_of(i)
        x = r_.xs[l, pl.ds(4 * half, 4)].reshape(W, D)
        r_.kvT[l, :, rows] = dot_nt(r_.wkvT[l], x).astype(BF16)

    def attention_heads(l, i, hfs):
        _, rows = half_of(i)
        for hf in hfs:
            lanes = lane_half(hf)
            ones = jnp.ones((HEAD_DIM, W), BF16)
            for c in range(HK // 2):
                r_.sc[c % 2, 0 : 2 * R] = dot(r_.qm[l, hf, 2 * c * R : 2 * (c + 1) * R], r_.kvT[l, lanes, rows])
                for k in range(2):
                    for at in range(0, R, STRIP):
                        s = r_.sc[c % 2, k * R + at : k * R + at + STRIP] + r_.bias[at : at + STRIP, rows]
                        top = jnp.max(s, 1, keepdims=True)
                        e = jnp.exp2((s - top) * factor_exp)
                        r_.tp[2 * c + k, at : at + STRIP] = jnp.broadcast_to(top, (STRIP, 128))
                        first = pl.multiple_of((hf * HK + 2 * c + k) * R + at, STRIP)
                        r_.pst[l, pl.ds(first, STRIP), rows] = e.astype(BF16)
                for k in range(2):
                    h = 2 * c + k
                    left = jnp.concatenate([r_.kvT[l, head_dims(hf, h, D), rows], ones], 0)
                    o = dot_nt(left, r_.pst[l, head_rows(hf, h), rows])
                    r_.odT[i, head_dims(hf, h)] = o[0:HEAD_DIM]
                    r_.ldT[i, head_dims(hf, h)] = o[HEAD_DIM:]
            r_.md[i, :, lanes] = by_head([r_.tp[k] for k in range(HK)])

    def attention_end(l):
        tops = [r_.md[i].T for i in range(NB)]
        top = tops[0]
        for i in range(1, NB):
            top = jnp.maximum(top, tops[i])
        factors = [jnp.exp2((tops[i] - top) * factor_exp) for i in range(NB)]
        inv = 1.0 / sum(factors[i] * r_.ldT[i] for i in range(NB))
        o = jnp.zeros((D, R), F32)
        for i in range(NB):
            r_.rb[l, i] = (factors[i] * inv).T
            o = o + factors[i] * inv * r_.odT[i]
        o = o.T
        r_.oraw[l] = o
        ob = o.astype(BF16)
        r_.ob[l] = ob
        t1 = r_.xf[l] + dot(ob, r_.wo[l])
        r_.z1[l] = t1
        mean1 = col_sum(t1) / R
        return mean1, col_sum((t1 - mean1) * (t1 - mean1))

    def convolution(l):
        xs = r_.xs
        xb = xs[l, me]
        r_.xe[l, 0:R] = xb
        r_.xe[l, R : R + 32] = dot(r_.HP[...], xs[l, prev]).astype(BF16)
        r_.xe[l, R + 32 : R + 64] = dot(r_.HN[...], xs[l, nxt]).astype(BF16)
        xe = r_.xe[l]
        made = dot(xe, r_.wp[l])
        pd_high, pd_low = split(made[:, 2 * D : 3 * D])
        r_.re[0:256] = made[:, 3 * D :].astype(BF16)
        r_.re[256:512] = r_.we[l]
        r_.re[512:768] = pd_high
        r_.re[768:1024] = pd_low
        r_.gate[l] = dot(r_.le[...], r_.re[...])
        r_.bs[l] = dot(r_.le[:, 0:256], made[:, D : 2 * D].astype(BF16)).astype(BF16)
        for at in range(0, E, 64):
            here = slice(at, at + 64)
            gate = sigmoid(r_.gate[l, here])
            r_.gate[l, here] = gate
            high, low = split(jnp.concatenate([gate * r_.bs[l, here].astype(F32), gate], 1))
            r_.gg[here] = high
            r_.gg[E + at : E + at + 64] = low
        num_den = dot(r_.TT[...], r_.gg[...])
        pa, num, den = made[0:R, 0:D], num_den[:, 0:D], num_den[:, D:]
        r_.num[l] = num
        r_.den[l] = den
        msg = pa + num / (den + GATE_EPS)
        r_.z0[l] = msg
        mean0 = col_sum(msg) / R
        return mean0, col_sum((msg - mean0) * (msg - mean0))

    def forward(l, carry):
        def ready(js):
            for j in js:
                moved = (r_.gb[l, j].astype(F32) + r_.moff[j, 0:1]) * r_.move[0:1] + r_.move[1:2]
                r_.xs[l, j] = moved.astype(BF16)

        r_.xs[l, me] = r_.xf[l].astype(BF16)
        prepare_queries(l)
        gather_near(l)
        ready([partner, 2 * z_from(1) + par, 2 * z_from(1) + 1 - par])

        attention_keys(l, 0)
        attention_heads(l, 0, (0,))
        for t in range(2, NZ):
            gather_pass(l, t)
        attention_heads(l, 0, (1,))
        gather_far(l)
        ready([2 * z_from(t) + p for t in range(2, NZ) for p in range(2)])
        mean0, sq0 = convolution(l)
        for i in range(1, NB):
            attention_keys(l, i)
            attention_heads(l, i, (0, 1))
        sync_start(3 * l, mean0, sq0)
        mean1, sq1 = attention_end(l)
        sync_start(3 * l + 1, mean1, sq1)
        mean0, sq0 = sync_moments(3 * l)
        inv0 = lax.rsqrt(sq0 / total + NORM_EPS)
        r_.iv[l, 0:1] = inv0
        z0 = (r_.z0[l] - mean0) * inv0
        r_.z0[l] = z0
        n0 = z0 * r_.gain[l, 0:1] + r_.shift[l, 0:1]
        r_.local[...] = r_.xf[l] + n0 * sigmoid(n0)
        mean1, sq1 = sync_moments(3 * l + 1)
        inv1 = lax.rsqrt(sq1 / total + NORM_EPS)
        r_.iv[l, 1:2] = inv1
        z1 = (r_.z1[l] - mean1) * inv1
        r_.z1[l] = z1
        mix = r_.local[...] + z1 * r_.gain[l, 1:2] + r_.shift[l, 1:2]
        mb = mix.astype(BF16)
        r_.mb[l] = mb
        u = dot(mb, r_.wu[l])
        r_.u[l] = u
        g = (u * sigmoid(u)).astype(BF16)
        r_.g[l] = g
        y = mix + dot(g, r_.wd[l])
        r_.z2[l] = y
        mean = col_sum(y) / R
        cent = y - mean
        k = 3 * l + 2
        sync_start(k, mean, col_sum(cent * cent))

        @pl.when(l < L - 1)
        def _():
            r_.gb[l + 1, me] = cent.astype(BF16)
            gather_start(l + 1)

        @pl.when(l == L - 1)
        def _():
            dy = r_.cot[...].astype(F32)
            sync_start(3 * L, col_sum(dy), col_sum(dy * cent))

        tot_mean, tot_sq = sync_moments(k)
        inv2 = lax.rsqrt(tot_sq / total + NORM_EPS)
        r_.iv[l, 2:3] = inv2
        z2 = (r_.z2[l] - tot_mean) * inv2
        r_.z2[l] = z2
        gain, shift = r_.gain[l, 2:3], r_.shift[l, 2:3]
        r_.xf[l + 1] = z2 * gain + shift

        @pl.when(l == L - 1)
        def _():
            sync_wait(3 * L)
            sums, means = r_.st1[3 * L], r_.st1[k][:, 0:2]
            mean = jnp.mean(means, 0)
            dy_sum = jnp.sum(sums[:, 0:2], 0)
            dy_cent = jnp.sum(sums[:, 2:4] + (means - mean) * sums[:, 0:2], 0)
            dy_sum, dy_cent = unpack(jnp.concatenate([dy_sum, dy_cent], 0))
            r_.gshift[l, 2:3] = dy_sum
            r_.ggain[l, 2:3] = dy_cent * inv2

        for j in range(N):
            tile = r_.st1[k, rep * N + j]
            r_.moff[j, 0:1] = jnp.concatenate([tile[0:1], tile[1:2]], 1) - tot_mean
        r_.move[0:1] = inv2 * gain
        r_.move[1:2] = shift
        return carry

    lax.fori_loop(0, L, forward, 0)
    act_copy = pltpu.make_async_copy(r_.xf.at[L], r_.out_act, r_.store.at[0])
    act_copy.start()

    def back_feed_forward(l, k):
        s2, g2 = r_.gshift[l, 2:3], r_.ggain[l, 2:3]
        d3 = r_.gain[l, 2:3] * r_.iv[l, 2:3] * (r_.dy[...] - s2 / total - r_.z2[l] * (g2 / total))
        db = d3.astype(BF16)
        dub = (dot_nt(db, r_.wd[l]) * silu_slope(r_.u[l])).astype(BF16)
        dmix = d3 + dot_nt(dub, r_.wu[l])
        r_.dmix[...] = dmix
        n0 = r_.z0[l] * r_.gain[l, 0:1] + r_.shift[l, 0:1]
        gy0 = dmix * silu_slope(n0)
        sync_start(k, col_sum(dmix), col_sum(dmix * r_.z1[l]))
        sync_start(k + 1, col_sum(gy0), col_sum(gy0 * r_.z0[l]))
        r_.gy0[...] = gy0
        at = put(r_.gs_early, l, 512, dot_tn(r_.mb[l], dub))
        put(r_.gs_early, l, at, dot_tn(r_.g[l], db))
        r_.xeT[...] = r_.xe[l].T
        r_.qT[...] = r_.q[l].T

    def back_norms(l, k):
        s1, g1 = sync_sums(k)
        r_.gshift[l, 1:2] = s1
        r_.ggain[l, 1:2] = g1
        dmix = r_.dmix[...]
        d2 = r_.gain[l, 1:2] * r_.iv[l, 1:2] * (dmix - s1 / total - r_.z1[l] * (g1 / total))
        dab = d2.astype(BF16)
        r_.dxo[...] = dmix + d2
        r_.dob[...] = dot_nt(dab, r_.wo[l]).astype(BF16).astype(F32)
        put(r_.gs_early, l, 0, dot_tn(r_.ob[l], dab))
        r_.gkv[...] = jnp.zeros((2 * D, D), F32)
        r_.dqT[...] = jnp.zeros((D, R), F32)

    def back_half(i):
        t1 = (i + 1) % NB
        half = (zh + t1) % NB
        return t1, half, pl.ds(pl.multiple_of(half * W, 128), W)

    def back_heads(l, i, hf):
        t1, half, rows = back_half(i)
        if True:
            lanes = lane_half(hf)
            dos = r_.dob[:, lanes] * r_.rb[l, (NB - t1) % NB, :, lanes]
            prod = dos * r_.oraw[l, :, lanes]
            for k in range(HK):
                r_.dom[k * R : (k + 1) * R, 0:128] = jnp.where(lane_head == k, dos, 0.0).astype(BF16)
                r_.dom[k * R : (k + 1) * R, 128:256] = jnp.where(lane_head == k, -prod, 0.0).astype(BF16)
            r_.dosT[...] = dos.T.astype(BF16)
            values = pl.ds(pl.multiple_of(D + hf * 128, 128), 128)
            right = jnp.concatenate([r_.kvT[l, values, rows], jnp.ones((128, W), BF16)], 0)
            for c in range(HK // 2):
                both = slice(2 * c * R, 2 * (c + 1) * R)
                r_.sc[c % 2, 0 : 2 * R] = dot(r_.dom[both], right)
                for k in range(2):
                    for at in range(0, R, STRIP):
                        first = pl.multiple_of((hf * HK + 2 * c + k) * R + at, STRIP)
                        e = r_.pst[l, pl.ds(first, STRIP), rows].astype(F32)
                        ds = e * r_.sc[c % 2, k * R + at : k * R + at + STRIP]
                        r_.dss[(2 * c + k) * R + at : (2 * c + k) * R + at + STRIP] = ds.astype(BF16)
                for k in range(2):
                    h = 2 * c + k
                    mine, dims = slice(h * R, (h + 1) * R), head_dims(hf, h)
                    r_.dqT[dims] += dot_nt(r_.kvT[l, dims, rows], r_.dss[mine])
                    r_.dkv[dims] = (dot(r_.qT[dims], r_.dss[mine]) * scale).astype(BF16)
                    dv = dot(r_.dosT[h * HEAD_DIM : (h + 1) * HEAD_DIM], r_.pst[l, head_rows(hf, h), rows])
                    r_.dkv[head_dims(hf, h, D)] = dv.astype(BF16)

    def back_rows(l, i):
        t1, half, rows = back_half(i)
        dx = dot(r_.wqkv[l, :, D:], r_.dkv[...]).T
        r_.dxs[l, pl.ds(2 * half, 2)] = dx.astype(BF16).reshape(2, 2, R, D)

        if i < NB - 1:
            for low in range(2):
                zb = 2 * half + low
                send_rows(r_.dxs.at[l, zb, 1 - par], r_.rs1.at[l, zb], R,
                     r_.rs_s.at[0], r_.rsp_r.at[l, i], nodes=partner)

        else:
            near = z_to(1)
            send_rows(r_.dxs.at[l, z, 1 - par], r_.ro.at[l, 0], R, r_.rs_s.at[0], r_.ro_r.at[l], nodes=partner)
            send_rows(r_.dxs.at[l, near, par], r_.ro.at[l, 1], R, r_.rs_s.at[0], r_.ro_r.at[l], nodes=2 * near + par)
            send_rows(r_.dxs.at[l, near, 1 - par], r_.ro.at[l, 2], R, r_.rs_s.at[0], r_.ro_r.at[l],
                 nodes=2 * near + 1 - par)

        r_.gkv[...] += dot(r_.dkv[...], r_.xs[l, pl.ds(4 * half, 4)].reshape(W, D))

    def pass_on(l, i, t):
        zb = z_to(t)
        if t % 2 == 0:
            arrive(r_.rs1.at[l, 0:2], r_.rsp_r.at[l, i])
        both = r_.dxs[l, zb, par].astype(F32) + r_.rs1[l, zb].astype(F32)
        r_.cs[l, zb] = both.astype(BF16)
        send_rows(r_.cs.at[l, zb], r_.rs2.at[l, z], R, r_.rs_s.at[0], r_.rsc_r.at[l], nodes=2 * zb + par)

    def back_convolution(l, k):
        s0, g0 = unpack(jnp.sum(r_.st1[k + 1], 0))
        r_.gshift[l, 0:1] = s0
        r_.ggain[l, 0:1] = g0
        inv_den = 1.0 / (r_.den[l] + GATE_EPS)
        dm = r_.gain[l, 0:1] * r_.iv[l, 0:1] * (r_.gy0[...] - s0 / total - r_.z0[l] * (g0 / total))
        dnum = dm * inv_den
        dden = -dnum * r_.num[l] * inv_den
        high, low = split(jnp.concatenate([dnum, dden], 1))
        r_.dn[0:R] = high
        r_.dn[256 : 256 + R] = low
        r_.sc[0, 0:E, 0 : 2 * D] = dot(r_.le[:, 512:1024], r_.dn[...])
        for at in range(0, E, 64):
            here = slice(at, at + 64)
            gate, dnum_e = r_.gate[l, here], r_.sc[0, here, 0:D]
            dgp = (dnum_e * r_.bs[l, here].astype(F32) + r_.sc[0, here, D : 2 * D]) * gate * (1.0 - gate)
            r_.gg[here, 0:D] = (dnum_e * gate).astype(BF16)
            r_.gg[here, D:] = dgp.astype(BF16)
        ext = dot(r_.ST[...], r_.gg[0:E]).astype(BF16)
        r_.dproj[0:R, 0:D] = dm.astype(BF16)
        r_.dproj[:, D : 2 * D] = ext[:, 0:D]
        r_.dproj[0:R, 2 * D : 3 * D] = dot(r_.TT[:, 0:E], r_.gg[0:E, D:]).astype(BF16)
        r_.dproj[:, 3 * D :] = ext[:, D:]
        dxe = dot_nt(r_.dproj[...], r_.wp[l])
        r_.hs[l, 0] = dxe[R : R + 32].astype(BF16)
        r_.hs[l, 1] = dxe[R + 32 : R + 64].astype(BF16)
        r_.dxo[...] += dxe[0:R]

    def send_halo(l):
        send(r_.hs.at[l, 0], r_.hr.at[l, 1], r_.hal_s.at[0], r_.hal_r.at[l], nodes=prev)
        send(r_.hs.at[l, 1], r_.hr.at[l, 0], r_.hal_s.at[0], r_.hal_r.at[l], nodes=nxt)

    def conv_weight_grads(l):
        at = put(r_.gs_conv, l, 0, dot(r_.xeT[...], r_.dproj[...]))
        put(r_.gs_conv, l, at, dot(r_.efT[...], r_.gg[0:E, D:]))

    def back_input(l):
        dx = r_.dxo[...]
        dx = dx + r_.dxs[l, z, par].astype(F32)
        arrive(r_.ro.at[l], r_.ro_r.at[l])
        for slot in range(3):
            dx = dx + r_.ro[l, slot].astype(F32)
        if NZ > 2:
            arrive(r_.rs2.at[l, 0 : NZ - 2], r_.rsc_r.at[l])
        for t in range(2, NZ):
            dx = dx + r_.rs2[l, z_from(t)].astype(F32)
        arrive(r_.hr.at[l], r_.hal_r.at[l])
        back = jnp.concatenate(
            [r_.hr[l, 0].astype(F32)[0:24], r_.hr[l, 1].astype(F32)[0:24], jnp.zeros((16, D), F32)], 0
        )
        return dx + dot(r_.A[...], back.astype(BF16))

    r_.dy[...] = r_.cot[...].astype(F32)

    E1, C1, Q1, E0, C0, QK0, V0 = range(len(GROUPS))

    def steps(*pairs):
        return [functools.partial(reduce_step, g, k) for g, k in pairs]

    r_.dy[...] = r_.cot[...].astype(F32)

    def backward(b, carry):
        l = L - 1 - b
        first, last = b == 0, b == L - 1
        k = 3 * L + 1 + 2 * b
        back_feed_forward(l, k)
        when(last, *steps((C1, 4), (Q1, 2), (E1, 6)))
        back_norms(l, k)
        sync_wait(k + 1)
        when(first, *steps((E1, 0)))
        when(last, *steps((C1, 5), (Q1, 3), (E0, 0)))
        back_convolution(l, k)
        back_heads(l, 0, 0)
        send_halo(l)
        when(first, *steps((E1, 1)))
        when(last, *steps((C1, 6), (Q1, 4), (E0, 1)))
        conv_weight_grads(l)
        back_heads(l, 0, 1)
        back_rows(l, 0)
        when(first, *steps((C1, 0), (E1, 2)))
        when(last, *steps((C0, 0), (E0, 2), (C1, 7), (Q1, 5)))
        back_heads(l, 1, 0)
        for t in range(2, NZ):
            pass_on(l, 0, t)
        when(first, *steps((C1, 1), (E1, 3)))
        when(last, *steps((C0, 1), (E0, 3), (C1, 8), (Q1, 6)))
        back_heads(l, 1, 1)
        back_rows(l, 1)
        when(first, *steps((C1, 2), (E1, 4)))
        when(last, *steps((C0, 2), (E0, 4)))
        dqb = (r_.dqT[...].T * scale).astype(BF16)
        r_.dxo[...] += dot_nt(dqb, r_.wqkv[l, :, 0:D])
        at = put(r_.gs_qkv, l, 0, dot(r_.xeT[:, 0:R], dqb))
        put(r_.gs_qkv, l, at, r_.gkv[...].T)
        when(first, *steps((Q1, 0)))

        @pl.when(first)
        def _():
            dx = back_input(l)
            r_.dy[...] = dx
            below = L - 2
            sync_start(SYNCS - 1, col_sum(dx), col_sum(dx * r_.z2[below]))
            for step in steps((C1, 3), (Q1, 1), (E1, 5)):
                step()
            s2, g2 = sync_sums(SYNCS - 1)
            r_.gshift[below, 2:3] = s2
            r_.ggain[below, 2:3] = g2

        return carry

    lax.fori_loop(0, L, backward, 0)
    for step in steps((QK0, 0), (V0, 0), (E0, 5), (C0, 3), (V0, 1), (QK0, 1)):
        step()
    r_.dy[...] = back_input(0)
    in_copy = pltpu.make_async_copy(r_.dy, r_.grad_in, r_.store.at[1])
    in_copy.start()
    for step in steps(
        (E0, 6), (C0, 4), (V0, 2), (QK0, 2),
        (E0, 7), (C0, 5), (V0, 3), (QK0, 3),
        (E0, 8), (C0, 6), (V0, 4), (QK0, 4),
    ):
        step()
    for l in range(L):
        for k in range(3):
            r_.ggain_out[k, l : l + 1] = r_.ggain[l, k : k + 1]
            r_.gshift_out[k, l : l + 1] = r_.gshift[l, k : k + 1]
    for g in range(len(GROUPS)):
        reduce_drain(g)
    sent(r_.meta.at[0 : N - 1], r_.meta_s.at[0])
    sent(r_.st1.at[:, 0 : M * N - 1], r_.st_s.at[0])
    sent(r_.gb.at[:, 0 : 3 + 2 * (NZ - 2)], r_.ag_s.at[0])
    sent(r_.gb.at[:, 0 : 2 * (NB - 1) + 3 + NZ - 2], r_.rs_s.at[0])
    sent(r_.hs, r_.hal_s.at[0])
    act_copy.wait()
    in_copy.wait()


def finish_kernel(act_h, gin_h, *refs):
    n = len(GROUPS)
    held, (ggain_h, gshift_h), refs = refs[:n], refs[n : n + 2], refs[n + 2 :]
    act_o, gin_o, proj_o, edge_o, qkv_o, out_o, up_o, down_o, ggain_o, gshift_o = refs[:10]
    summed, refs = refs[10 : 10 + n], refs[10 + n :]
    act, gin, proj, edge, qkv, out, up, down, in_sem, out_sem = refs
    loads = [
        pltpu.make_async_copy(src, dst, in_sem.at[i])
        for i, (src, dst) in enumerate(zip(held + (act_h, gin_h), summed + (act, gin), strict=True))
    ]
    for load in loads:
        load.start()
    ggain_o[...] = ggain_h[...]
    gshift_o[...] = gshift_h[...]
    stores = []

    def store(src, dst):
        copy = pltpu.make_async_copy(src, dst, out_sem.at[len(stores)])
        copy.start()
        stores.append(copy)

    def widen(dst, l, g, at, first=0, last=None):
        rows = dst.shape[1]
        for c in range(first, dst.shape[2] // 128 if last is None else last):
            dst[l, :, 128 * c : 128 * (c + 1)] = summed[g][at : at + rows].astype(F32)
            at += rows
        return at

    for g, (name, l, first, rows, _) in enumerate(GROUPS):
        loads[g].wait()
        if name == "early":
            at = widen(out, l, g, 0)
            store(out.at[l], out_o.at[l])
            at = widen(up, l, g, at)
            store(up.at[l], up_o.at[l])
            widen(down, l, g, at)
            store(down.at[l], down_o.at[l])
        elif name == "conv":
            at = widen(proj, l, g, 0)
            store(proj.at[l], proj_o.at[l])
            widen(edge, l, g, at)
            store(edge.at[l], edge_o.at[l])
        else:
            widen(qkv, l, g, 0, first // 256, (first + rows) // 256)
            if first + rows == 1536:
                store(qkv.at[l], qkv_o.at[l])
    for i, (src, dst) in enumerate(((act, act_o), (gin, gin_o))):
        loads[n + i].wait()
        store(src, dst)
    for copy in stores:
        copy.wait()


def fused_device(
    N, M, node_input, edge_feat, graph_ids, edge_src, edge_dst, halo_send, w_proj, w_edge, w_qkv,
    w_out, w_up, w_down, norm_gain, norm_shift, cotangent,
):
    R, D = node_input.shape
    E = edge_feat.shape[0]
    L = w_proj.shape[0]
    names = scratch_list(N, M, L, R, E)
    vmem = pl.BlockSpec(memory_space=pltpu.VMEM)
    hbm = pl.BlockSpec(memory_space=pltpu.HBM)
    shape = jax.ShapeDtypeStruct
    rows = shape((R, D), F32)
    norm = shape((3, L, D), F32)
    groups = [shape((rows_g, 128), BF16) for _, _, _, rows_g, _ in GROUPS]
    outs = pl.pallas_call(
        functools.partial(kernel, N, M, L, tuple(names)),
        out_shape=[rows, rows, *groups, norm, norm],
        in_specs=[hbm] + [vmem] * 4 + [hbm] * 7 + [vmem] * 2 + [hbm],
        out_specs=[hbm] * (2 + len(GROUPS)) + [vmem] * 2,
        scratch_shapes=list(names.values()),
        compiler_params=pltpu.CompilerParams(
            collective_id=0, has_side_effects=True, vmem_limit_bytes=60 << 20
        ),
        name="layers",
    )(node_input, graph_ids, edge_src, edge_dst, halo_send, edge_feat, w_proj, w_edge, w_qkv, w_out, w_up,
      w_down, norm_gain.transpose(1, 0, 2), norm_shift.transpose(1, 0, 2), cotangent)
    weights = [shape(w.shape, F32) for w in (w_proj, w_edge, w_qkv, w_out, w_up, w_down)]
    results = pl.pallas_call(
        finish_kernel,
        out_shape=[rows, rows, *weights, norm, norm],
        in_specs=[hbm] * (2 + len(GROUPS)) + [vmem] * 2,
        out_specs=[hbm] * 8 + [vmem] * 2,
        scratch_shapes=[pltpu.VMEM(s.shape, s.dtype) for s in (*groups, rows, rows, *weights)]
        + [pltpu.SemaphoreType.DMA((len(GROUPS) + 2,)), pltpu.SemaphoreType.DMA((14,))],
        compiler_params=pltpu.CompilerParams(vmem_limit_bytes=60 << 20),
        name="gradients",
    )(*outs)
    ggain, gshift = results[8].transpose(1, 0, 2), results[9].transpose(1, 0, 2)
    return (*results[:8], ggain, gshift)


BLOCK_CAP = 2048


def extended_2(block, sides, width):
    for axis, dim in sides:
        count = lax.axis_size(axis)
        forward = [(i, i + 1) for i in range(count - 1)]
        forward.append((count - 1, 0))
        backward = [(target, source) for source, target in forward]
        low = lax.ppermute(
            lax.slice_in_dim(block, block.shape[dim] - width, None, axis=dim), axis, forward
        )
        high = lax.ppermute(lax.slice_in_dim(block, 0, width, axis=dim), axis, backward)
        block = jnp.concatenate([low, block, high], axis=dim)
    return block


def block_length(total_rows, upper_limit):
    for length in range(min(total_rows, upper_limit), 0, -1):
        if total_rows % length == 0:
            return length
    return 1


def outer_product(left, right):
    return lax.dot_general(
        left, right, (((0,), (0,)), ((), ())), preferred_element_type=jnp.float32
    )


def times_transposed(left, weight):
    return lax.dot_general(
        left, weight, (((1,), (1,)), ((), ())), preferred_element_type=jnp.float32
    )


def forward_product(left, weight):
    return jnp.dot(left, weight, preferred_element_type=jnp.float32)


def silu_slope_plain(inputs):
    logistic = jax.nn.sigmoid(inputs)
    return logistic * (1.0 + inputs * (1.0 - logistic))


def normalize(inputs, gain_row, shift_row, node_total):
    batch_mean = lax.psum(jnp.sum(inputs, 0), ("nodes", "rep")) / node_total
    centred = inputs - batch_mean
    batch_var = lax.psum(jnp.sum(centred * centred, 0), ("nodes", "rep")) / node_total
    inv_std = lax.rsqrt(batch_var + NORM_EPS)
    standard = (inputs - batch_mean) * inv_std
    return (standard * gain_row + shift_row, standard, inv_std)


def normalize_back(grad_out, standard, inv_std, gain_row, node_total):
    shift_grad, gain_grad = lax.psum(
        (jnp.sum(grad_out, 0), jnp.sum(grad_out * standard, 0)), ("nodes", "rep")
    )
    grad_in = (
        gain_row
        * inv_std
        * (grad_out - shift_grad / node_total - standard * gain_grad / node_total)
    )
    return (grad_in, gain_grad, shift_grad)


def exchange_sources(outgoing):
    halo_rows = outgoing.shape[0] // 2
    grown = extended_2(outgoing, (("nodes", 0),), halo_rows)
    return jnp.concatenate([grown[:halo_rows], grown[3 * halo_rows :]], 0)


def return_sources(incoming_grad):
    halo_rows = incoming_grad.shape[0] // 2
    grown = extended_2(incoming_grad.astype(jnp.bfloat16), (("nodes", 0),), halo_rows).astype(
        incoming_grad.dtype
    )
    return jnp.concatenate([grown[:halo_rows], grown[3 * halo_rows :]], 0)


def attend_forward(query_rows, key_rows, value_rows, local_graphs, group_graphs):
    row_count = query_rows.shape[0]
    score_scale = HEAD_DIM ** (-0.5)
    queries = query_rows.reshape(row_count, HEADS, HEAD_DIM)

    def add_piece(carried, kv_piece, first_row):
        key_piece, value_piece = kv_piece
        piece_rows = key_piece.shape[0]
        block_len = block_length(piece_rows, BLOCK_CAP)

        def add_block(block_state, block_index):
            row_max, row_sum, accumulated = block_state
            block_start = block_index * block_len
            key_block = lax.dynamic_slice_in_dim(key_piece, block_start, block_len, 0).reshape(
                block_len, HEADS, HEAD_DIM
            )
            value_block = lax.dynamic_slice_in_dim(value_piece, block_start, block_len, 0).reshape(
                block_len, HEADS, HEAD_DIM
            )
            key_graphs = lax.dynamic_slice_in_dim(
                group_graphs, first_row + block_start, block_len, 0
            )
            same_graph = (local_graphs[:, None] == key_graphs[None, :])[None]
            scores = (
                jnp.einsum("qhd,khd->hqk", queries, key_block, preferred_element_type=jnp.float32)
                * score_scale
            )
            scores = jnp.where(same_graph, scores, NEG)
            new_max = jnp.maximum(row_max, jnp.max(scores, 2))
            weights = jnp.where(same_graph, jnp.exp(scores - new_max[:, :, None]), 0.0)
            factor = jnp.exp(row_max - new_max)
            row_sum = row_sum * factor + jnp.sum(weights, 2)
            contrib = jnp.einsum(
                "hqk,khd->qhd",
                weights.astype(jnp.bfloat16),
                value_block,
                preferred_element_type=jnp.float32,
            )
            accumulated = accumulated * jnp.transpose(factor)[:, :, None] + contrib
            return ((new_max, row_sum, accumulated), None)

        carried, _ = lax.scan(add_block, carried, jnp.arange(piece_rows // block_len))
        return carried

    start_state = (
        jnp.full((HEADS, row_count), NEG, jnp.float32),
        jnp.zeros((HEADS, row_count), jnp.float32),
        jnp.zeros((row_count, HEADS, HEAD_DIM), jnp.float32),
    )
    row_max, row_sum, accumulated = add_piece(
        start_state,
        (
            lax.all_gather(key_rows, "nodes", axis=0, tiled=True),
            lax.all_gather(value_rows, "nodes", axis=0, tiled=True),
        ),
        jnp.int32(0),
    )
    attn_raw = accumulated / jnp.transpose(row_sum)[:, :, None]
    log_sum = row_max + jnp.log(row_sum)
    return (attn_raw, log_sum)


def attend_backward(
    query_rows, key_rows, value_rows, grad_low, attn_raw, log_sum, local_graphs, group_graphs
):
    row_count = query_rows.shape[0]
    model_width = HEADS * HEAD_DIM
    score_scale = HEAD_DIM ** (-0.5)
    queries = query_rows.reshape(row_count, HEADS, HEAD_DIM)
    grad_heads = grad_low.reshape(row_count, HEADS, HEAD_DIM)
    row_delta = jnp.einsum("qhd,qhd->hq", grad_heads.astype(jnp.float32), attn_raw)

    def score_block(key_block, value_block, key_graphs):
        same_graph = (local_graphs[:, None] == key_graphs[None, :])[None]
        scores = (
            jnp.einsum("qhd,khd->hqk", queries, key_block, preferred_element_type=jnp.float32)
            * score_scale
        )
        attn_weights = jnp.exp(jnp.where(same_graph, scores - log_sum[:, :, None], NEG))
        grad_weights = jnp.einsum(
            "qhd,khd->hqk", grad_heads, value_block, preferred_element_type=jnp.float32
        )
        grad_scores = (attn_weights * (grad_weights - row_delta[:, :, None])).astype(jnp.bfloat16)
        return (attn_weights, grad_scores)

    def key_terms(attn_weights, grad_scores, block_len):
        grad_keys = (
            jnp.einsum("hqk,qhd->khd", grad_scores, queries, preferred_element_type=jnp.float32)
            * score_scale
        )
        grad_values = jnp.einsum(
            "hqk,qhd->khd",
            attn_weights.astype(jnp.bfloat16),
            grad_heads,
            preferred_element_type=jnp.float32,
        )
        return jnp.concatenate(
            [
                grad_keys.reshape(block_len, model_width),
                grad_values.reshape(block_len, model_width),
            ],
            1,
        )

    def query_term(grad_scores, key_block):
        return (
            jnp.einsum("hqk,khd->qhd", grad_scores, key_block, preferred_element_type=jnp.float32)
            * score_scale
        )

    group_rows = group_graphs.shape[0]

    def add_piece(carried, kv_piece, first_row):
        key_piece, value_piece = kv_piece
        piece_rows = key_piece.shape[0]
        block_len = block_length(piece_rows, BLOCK_CAP)

        def add_block(block_state, block_index):
            grad_query, buffer = block_state
            block_start = block_index * block_len
            key_block = lax.dynamic_slice_in_dim(key_piece, block_start, block_len, 0).reshape(
                block_len, HEADS, HEAD_DIM
            )
            value_block = lax.dynamic_slice_in_dim(value_piece, block_start, block_len, 0).reshape(
                block_len, HEADS, HEAD_DIM
            )
            place = first_row + block_start
            key_graphs = lax.dynamic_slice_in_dim(group_graphs, place, block_len, 0)
            attn_weights, grad_scores = score_block(key_block, value_block, key_graphs)
            grad_query = grad_query + query_term(grad_scores, key_block)
            block_terms = key_terms(attn_weights, grad_scores, block_len)
            current = lax.dynamic_slice_in_dim(buffer, place, block_len, 0)
            buffer = lax.dynamic_update_slice_in_dim(buffer, current + block_terms, place, 0)
            return ((grad_query, buffer), None)

        carried, _ = lax.scan(add_block, carried, jnp.arange(piece_rows // block_len))
        return carried

    start_state = (
        jnp.zeros((row_count, HEADS, HEAD_DIM), jnp.float32),
        jnp.zeros((group_rows, 2 * model_width), jnp.float32),
    )
    grad_query, buffer = add_piece(
        start_state,
        (
            lax.all_gather(key_rows, "nodes", axis=0, tiled=True),
            lax.all_gather(value_rows, "nodes", axis=0, tiled=True),
        ),
        jnp.int32(0),
    )
    grad_kv = lax.psum_scatter(buffer, "nodes", scatter_dimension=0, tiled=True)
    return (
        grad_query.reshape(row_count, model_width),
        grad_kv[:, :model_width],
        grad_kv[:, model_width:],
    )


def layer_forward(
    hidden, params, edge_feat, edge_src, edge_dst, halo_send, local_graphs, group_graphs, node_total
):
    w_proj, w_edge, w_qkv, w_out, w_up, w_down, norm_gains, norm_shifts = params
    row_count, model_width = hidden.shape
    hidden_low = hidden.astype(jnp.bfloat16)
    projected = forward_product(hidden_low, w_proj)
    self_term = projected[:, :model_width]
    dest_term = projected[:, 2 * model_width : 3 * model_width]
    source_rows = jnp.concatenate(
        [projected[:, model_width : 2 * model_width], projected[:, 3 * model_width :]], 1
    ).astype(jnp.bfloat16)
    incoming = exchange_sources(source_rows[halo_send])
    extended = jnp.concatenate([source_rows, incoming], 0)
    edge_rows = extended[edge_src].astype(jnp.float32)
    source_b = edge_rows[:, :model_width]
    source_e = edge_rows[:, model_width:]
    edge_proj = forward_product(edge_feat, w_edge)
    gating = jax.nn.sigmoid(dest_term[edge_dst] + source_e + edge_proj)
    numerator = jax.ops.segment_sum(gating * source_b, edge_dst, row_count)
    denominator = jax.ops.segment_sum(gating, edge_dst, row_count)
    message = self_term + numerator / (denominator + GATE_EPS)
    normed_one, standard_one, inv_one = normalize(
        message, norm_gains[0], norm_shifts[0], node_total
    )
    local_out = hidden + jax.nn.silu(normed_one)
    qkv_low = forward_product(hidden_low, w_qkv).astype(jnp.bfloat16)
    query_rows = qkv_low[:, :model_width]
    key_rows = qkv_low[:, model_width : 2 * model_width]
    value_rows = qkv_low[:, 2 * model_width :]
    attn_raw, log_sum = attend_forward(query_rows, key_rows, value_rows, local_graphs, group_graphs)
    attn_low = attn_raw.reshape(row_count, model_width).astype(jnp.bfloat16)
    attn_proj = forward_product(attn_low, w_out)
    normed_two, standard_two, inv_two = normalize(
        hidden + attn_proj, norm_gains[1], norm_shifts[1], node_total
    )
    mixed = local_out + normed_two
    mixed_low = mixed.astype(jnp.bfloat16)
    up_proj = forward_product(mixed_low, w_up)
    activated = jax.nn.silu(up_proj).astype(jnp.bfloat16)
    down_proj = forward_product(activated, w_down)
    normed_three, standard_three, inv_three = normalize(
        mixed + down_proj, norm_gains[2], norm_shifts[2], node_total
    )
    saved = (
        hidden_low,
        source_b,
        gating,
        numerator,
        denominator,
        normed_one,
        standard_one,
        inv_one,
        query_rows,
        key_rows,
        value_rows,
        attn_raw,
        log_sum,
        attn_low,
        standard_two,
        inv_two,
        mixed_low,
        up_proj,
        activated,
        standard_three,
        inv_three,
    )
    return (normed_three, saved)


def layer_backward(
    grad_out,
    params,
    saved,
    edge_feat,
    edge_src,
    edge_dst,
    halo_send,
    local_graphs,
    group_graphs,
    node_total,
):
    w_proj, w_edge, w_qkv, w_out, w_up, w_down, norm_gains, norm_shifts = params
    (
        hidden_low,
        source_b,
        gating,
        numerator,
        denominator,
        normed_one,
        standard_one,
        inv_one,
        query_rows,
        key_rows,
        value_rows,
        attn_raw,
        log_sum,
        attn_low,
        standard_two,
        inv_two,
        mixed_low,
        up_proj,
        activated,
        standard_three,
        inv_three,
    ) = saved
    row_count, model_width = grad_out.shape
    grad_three, gain_three, shift_three = normalize_back(
        grad_out, standard_three, inv_three, norm_gains[2], node_total
    )
    down_grad = grad_three.astype(jnp.bfloat16)
    grad_w_down = outer_product(activated, down_grad)
    up_grad = (times_transposed(down_grad, w_down) * silu_slope_plain(up_proj)).astype(jnp.bfloat16)
    grad_w_up = outer_product(mixed_low, up_grad)
    grad_mixed = grad_three + times_transposed(up_grad, w_up)
    grad_two, gain_two, shift_two = normalize_back(
        grad_mixed, standard_two, inv_two, norm_gains[1], node_total
    )
    out_grad = grad_two.astype(jnp.bfloat16)
    grad_w_out = outer_product(attn_low, out_grad)
    attn_grad = times_transposed(out_grad, w_out).astype(jnp.bfloat16)
    grad_query, grad_key, grad_value = attend_backward(
        query_rows, key_rows, value_rows, attn_grad, attn_raw, log_sum, local_graphs, group_graphs
    )
    qkv_grad = jnp.concatenate([grad_query, grad_key, grad_value], 1).astype(jnp.bfloat16)
    grad_w_qkv = outer_product(hidden_low, qkv_grad)
    grad_message, gain_one, shift_one = normalize_back(
        grad_mixed * silu_slope_plain(normed_one), standard_one, inv_one, norm_gains[0], node_total
    )
    shifted = denominator + GATE_EPS
    grad_numer = grad_message / shifted
    grad_denom = -grad_message * numerator / (shifted * shifted)
    numer_edge = grad_numer[edge_dst]
    grad_gate = numer_edge * source_b + grad_denom[edge_dst]
    grad_pre_edge = grad_gate * gating * (1.0 - gating)
    edge_grad = grad_pre_edge.astype(jnp.bfloat16)
    grad_w_edge = outer_product(edge_feat, edge_grad)
    grad_dest = jax.ops.segment_sum(grad_pre_edge, edge_dst, row_count)
    grad_extended = jax.ops.segment_sum(
        jnp.concatenate([numer_edge * gating, grad_pre_edge], 1),
        edge_src,
        row_count + halo_send.shape[0],
    )
    returned = return_sources(grad_extended[row_count:])
    grad_source = grad_extended[:row_count].at[halo_send].add(returned)
    proj_grad = jnp.concatenate(
        [grad_message, grad_source[:, :model_width], grad_dest, grad_source[:, model_width:]], 1
    ).astype(jnp.bfloat16)
    grad_w_proj = outer_product(hidden_low, proj_grad)
    grad_hidden = (
        grad_mixed
        + grad_two
        + times_transposed(proj_grad, w_proj)
        + times_transposed(qkv_grad, w_qkv)
    )
    weight_grads = (grad_w_proj, grad_w_edge, grad_w_qkv, grad_w_out, grad_w_up, grad_w_down)
    return (
        grad_hidden,
        weight_grads,
        jnp.stack([gain_one, gain_two, gain_three]),
        jnp.stack([shift_one, shift_two, shift_three]),
    )


def per_device(
    node_input,
    edge_feat,
    graph_ids,
    edge_src,
    edge_dst,
    halo_send,
    w_proj,
    w_edge,
    w_qkv,
    w_out,
    w_up,
    w_down,
    norm_gain,
    norm_shift,
    cotangent,
):
    group_graphs = lax.all_gather(graph_ids, "nodes", axis=0, tiled=True)
    node_total = node_input.shape[0] * lax.axis_size("nodes") * lax.axis_size("rep")
    layer_count = w_proj.shape[0]
    layer_params = [
        (
            w_proj[layer_index],
            w_edge[layer_index],
            w_qkv[layer_index],
            w_out[layer_index],
            w_up[layer_index],
            w_down[layer_index],
            norm_gain[layer_index],
            norm_shift[layer_index],
        )
        for layer_index in range(layer_count)
    ]
    hidden = node_input.astype(jnp.float32)
    saved_all = []
    for layer_index in range(layer_count):
        hidden, saved = layer_forward(
            hidden,
            layer_params[layer_index],
            edge_feat,
            edge_src,
            edge_dst,
            halo_send,
            graph_ids,
            group_graphs,
            node_total,
        )
        saved_all.append(saved)
    grad_hidden = cotangent.astype(jnp.float32)
    weight_parts = [None] * layer_count
    gain_parts = [None] * layer_count
    shift_parts = [None] * layer_count
    for layer_index in range(layer_count - 1, -1, -1):
        (
            grad_hidden,
            weight_parts[layer_index],
            gain_parts[layer_index],
            shift_parts[layer_index],
        ) = layer_backward(
            grad_hidden,
            layer_params[layer_index],
            saved_all[layer_index],
            edge_feat,
            edge_src,
            edge_dst,
            halo_send,
            graph_ids,
            group_graphs,
            node_total,
        )
    proj_local = jnp.stack([weight_parts[layer_index][0] for layer_index in range(layer_count)])
    edge_local = jnp.stack([weight_parts[layer_index][1] for layer_index in range(layer_count)])
    qkv_local = jnp.stack([weight_parts[layer_index][2] for layer_index in range(layer_count)])
    out_local = jnp.stack([weight_parts[layer_index][3] for layer_index in range(layer_count)])
    up_local = jnp.stack([weight_parts[layer_index][4] for layer_index in range(layer_count)])
    down_local = jnp.stack([weight_parts[layer_index][5] for layer_index in range(layer_count)])
    grad_proj, grad_edge, grad_qkv, grad_out, grad_up, grad_down = lax.psum(
        (proj_local, edge_local, qkv_local, out_local, up_local, down_local), ("nodes", "rep")
    )
    return (
        hidden,
        grad_hidden,
        grad_proj,
        grad_edge,
        grad_qkv,
        grad_out,
        grad_up,
        grad_down,
        jnp.stack(gain_parts),
        jnp.stack(shift_parts),
    )


def solution(mesh):
    in_specs = (
        P(("rep", "nodes"), None),
        P(("rep", "nodes"), None),
        P(("rep", "nodes")),
        P(("rep", "nodes")),
        P(("rep", "nodes")),
        P(("rep", "nodes")),
        P(),
        P(),
        P(),
        P(),
        P(),
        P(),
        P(),
        P(),
        P(("rep", "nodes"), None),
    )
    out_specs = (
        P(("rep", "nodes"), None),
        P(("rep", "nodes"), None),
        P(),
        P(),
        P(),
        P(),
        P(),
        P(),
        P(),
        P(),
    )
    N, M = mesh.shape["nodes"], mesh.shape["rep"]
    fused = N in (4, 8) and M % 2 == 0 and 512 % (16 * N * M) == 0
    return jax.shard_map(
        functools.partial(fused_device, N, M) if fused else per_device,
        mesh=mesh, in_specs=in_specs, out_specs=out_specs, check_vma=False,
    )
```

```python
import functools
import math

import jax
import jax.numpy as jnp
from jax import lax
from jax.experimental import pallas as pl
from jax.experimental.pallas import tpu as pltpu
from jax.sharding import PartitionSpec as P

HEADS = 8
HEAD_DIM = 32
NEG = -1e30
NORM_EPS = 1e-05
GATE_EPS = 1e-06
F32, BF16, I32 = jnp.float32, jnp.bfloat16, jnp.int32
MESH = pl.DeviceIdType.MESH
SYNCS = 12
STRIP = 32
GROUPS = (
    ("early", 1, 0, 2560, ("core", "y", "nodes")),
    ("conv", 1, 0, 2560, ("core", "x", "y", "z")),
    ("qkv", 1, 0, 1536, ("core", "y", "nodes")),
    ("early", 0, 0, 2560, ("core", "x", "y", "z")),
    ("conv", 0, 0, 2560, ("core", "y", "nodes")),
    ("qkv", 0, 0, 1024, ("rep", "nodes")),
    ("qkv", 0, 1024, 512, ("nodes", "rep")),
)


def dot(left, right):
    return lax.dot_general(
        left, right, (((1,), (0,)), ((), ())), preferred_element_type=F32
    )


def dot_nt(left, right):
    return lax.dot_general(
        left, right, (((1,), (1,)), ((), ())), preferred_element_type=F32
    )


def dot_tn(left, right):
    return lax.dot_general(
        left, right, (((0,), (0,)), ((), ())), preferred_element_type=F32
    )


def split(value):
    high = value.astype(BF16)
    return high, (value - high.astype(F32)).astype(BF16)


def sigmoid(value):
    return jax.nn.sigmoid(value)


def silu_slope(value):
    logistic = sigmoid(value)
    return logistic * (1.0 + value * (1.0 - logistic))


def col_sum(value):
    return jnp.sum(value, axis=0, keepdims=True)


def pack(first, second):
    return jnp.concatenate([first[:, :128], first[:, 128:], second[:, :128], second[:, 128:]], 0)


def unpack(tile):
    return [jnp.concatenate([tile[i : i + 1], tile[i + 1 : i + 2]], 1) for i in (0, 2)]


def combine_moments(tiles, count):
    mean = jnp.mean(tiles[:, 0:2], 0)
    off = tiles[:, 0:2] - mean
    return jnp.concatenate([mean, jnp.sum(tiles[:, 2:4] + count * off * off, 0)], 0)


class Refs:
    pass


def axis_sizes(N, M):
    return dict(core=2, y=M // 2, x=2, z=N // 2, rep=M, nodes=N)


def scratch_list(N, M, L, R, E):
    NZ, NB, G = N // 2, N // 4, N * R
    D, FF, W, HH = 256, 512, 4 * R, HEADS // 2 * R
    dma = lambda *shape: pltpu.SemaphoreType.DMA(shape)
    vm = lambda dtype, *shape: pltpu.VMEM(shape, dtype)
    names = dict(
        gb=vm(BF16, L, N, R, D),
        xs=vm(BF16, L, N, R, D),
        meta=vm(I32, N, 8, 256),
        cot=vm(BF16, R, D),
        wp=vm(BF16, L, D, 4 * D),
        we=vm(BF16, L, D, D),
        wqkv=vm(BF16, L, D, 3 * D),
        wo=vm(BF16, L, D, D),
        wu=vm(BF16, L, D, FF),
        wd=vm(BF16, L, FF, D),
        st1=vm(F32, SYNCS, M * N, 4, 128),
        gain=vm(F32, L, 8, D),
        shift=vm(F32, L, 8, D),
        ggain=vm(F32, L, 8, D),
        gshift=vm(F32, L, 8, D),
        iv=vm(F32, L, 8, D),
        moff=vm(F32, N, 8, D),
        move=vm(F32, 8, D),
        le=vm(BF16, E, 1024),
        re=vm(BF16, 1024, D),
        TT=vm(BF16, R, 2 * E),
        ST=vm(BF16, 256, E),
        efT=vm(BF16, D, E),
        HP=vm(BF16, 32, R),
        HN=vm(BF16, 32, R),
        A=vm(BF16, R, 64),
        bias=vm(F32, R, G),
        xf=vm(F32, L + 1, R, D),
        xe=vm(BF16, L, 256, D),
        xeT=vm(BF16, D, 256),
        gate=vm(F32, L, E, D),
        bs=vm(BF16, L, E, D),
        num=vm(F32, L, R, D),
        den=vm(F32, L, R, D),
        z0=vm(F32, L, R, D),
        z1=vm(F32, L, R, D),
        z2=vm(F32, L, R, D),
        wkvT=vm(BF16, L, 2 * D, D),
        kvT=vm(BF16, L, 2 * D, G),
        odT=vm(F32, NB, D, R),
        ldT=vm(F32, NB, D, R),
        md=vm(F32, NB, R, D),
        rb=vm(F32, L, NB, R, D),
        pst=vm(BF16, L, HEADS * R, G),
        oraw=vm(F32, L, R, D),
        ob=vm(BF16, L, R, D),
        mb=vm(BF16, L, R, D),
        u=vm(F32, L, R, FF),
        g=vm(BF16, L, R, FF),
        dy=vm(F32, R, D),
        dmix=vm(F32, R, D),
        gy0=vm(F32, R, D),
        local=vm(F32, R, D),
        dxo=vm(F32, R, D),
        dob=vm(F32, R, D),
        dqT=vm(F32, D, R),
        qm=vm(BF16, L, 2, HH, 128),
        q=vm(BF16, L, R, D),
        qT=vm(BF16, D, R),
        dosT=vm(BF16, 128, R),
        dom=vm(BF16, HH, 256),
        sc=vm(F32, 2, max(2 * R, E), W),
        tp=vm(F32, HEADS // 2, R, 128),
        dss=vm(BF16, HH, W),
        dkv=vm(BF16, 2 * D, W),
        gkv=vm(F32, 2 * D, D),
        gg=vm(BF16, 2 * E, 2 * D),
        dn=vm(BF16, 512, 2 * D),
        dproj=vm(BF16, 256, 4 * D),
        dxs=vm(BF16, L, NZ, 2, R, D),
        rs1=vm(BF16, L, NZ, R, D),
        cs=vm(BF16, L, NZ, R, D),
        rs2=vm(BF16, L, NZ, R, D),
        ro=vm(BF16, L, 3, R, D),
        hs=vm(BF16, L, 2, 32, D),
        hr=vm(BF16, L, 2, 32, D),
    )
    names.update(
        gs_early=vm(BF16, L, 2560, 128),
        gs_conv=vm(BF16, L, 2560, 128),
        gs_qkv=vm(BF16, L, 1536, 128),
    )
    sizes = axis_sizes(N, M)
    for g, (_, _, _, rows, stages) in enumerate(GROUPS):
        names[f"go{g}"] = vm(BF16, rows, 128)
        left = rows
        for k, axis in enumerate(stages):
            left //= sizes[axis]
            names[f"ga{g}_{k}"] = vm(BF16, sizes[axis] - 1, left, 128)
            if k < len(stages) - 1:
                names[f"gh{g}_{k}"] = vm(BF16, left, 128)
    names.update(
        ar_s=dma(len(GROUPS)),
        ar_r=dma(sum(2 * len(stages) for *_, stages in GROUPS)),
        ar_l=dma(len(GROUPS)),
        load=dma(9),
        store=dma(2),
        meta_s=dma(1),
        meta_r=dma(1),
        st_s=dma(1),
        st_r=dma(SYNCS),
        ag_s=dma(1),
        agn_r=dma(L),
        agc_r=dma(L, NZ),
        agp_r=dma(L),
        rs_s=dma(1),
        rsp_r=dma(L, NB),
        ro_r=dma(L),
        rsc_r=dma(L),
        hal_s=dma(1),
        hal_r=dma(L),
    )
    return names


IN_NAMES = (
    "x_in", "ids", "edge_src", "edge_dst", "halo", "ef_h", "wp_h", "we_h", "wqkv_h", "wo_h", "wu_h", "wd_h",
    "gain_in", "shift_in", "cot_h",
)
OUT_NAMES = ("out_act", "grad_in", *(f"gout{g}" for g in range(len(GROUPS))), "ggain_out", "gshift_out")


def kernel(N, M, L, names, *args):
    r_ = Refs()
    for name, ref in zip(IN_NAMES + OUT_NAMES + tuple(names), args, strict=True):
        setattr(r_, name, ref)
    R, D = r_.x_in.shape
    E = r_.ef_h.shape[0]
    NZ, NB, G, W = N // 2, N // 4, N * R, 4 * R
    HK = HEADS // 2
    total = float(N * M * R)
    scale = HEAD_DIM ** -0.5
    me = lax.axis_index("nodes")
    rep = lax.axis_index("rep")
    z = me // 2
    par = me % 2
    partner = 2 * z + (1 - par)
    prev = (me + N - 1) % N
    nxt = (me + 1) % N
    zh, zl = z // 2, z % 2
    z_to = lambda t: 2 * ((zh + t // 2) % NB) + (zl + t % 2) % 2
    z_from = lambda t: 2 * ((zh + NB - t // 2) % NB) + (zl + t % 2) % 2

    def remote(src, dst, s_sem, r_sem, **where):
        return pltpu.make_async_remote_copy(
            src_ref=src, dst_ref=dst, send_sem=s_sem, recv_sem=r_sem,
            device_id=where, device_id_type=MESH,
        )

    def send(src, dst, s_sem, r_sem, **where):
        remote(src, dst, s_sem, r_sem, **where).start()

    def send_rows(src, dst, rows, s_sem, r_sem, **where):
        pieces = next(p for p in range(1, rows) if rows % (16 * p) == 0 and rows // p <= 128)
        for at in range(0, rows, rows // pieces):
            cut = pl.ds(at, rows // pieces)
            send(src.at[cut], dst.at[cut], s_sem, r_sem, **where)

    def arrive(dst, r_sem):
        remote(dst, dst, r_sem, r_sem, nodes=partner).wait_recv()

    def sent(src, s_sem):
        remote(src, src, s_sem, s_sem, nodes=partner).wait_send()

    def when(condition, *acts):
        if condition:
            for act in acts:
                act()

    loads = [pltpu.make_async_copy(r_.ef_h, r_.le.at[:, D : 2 * D], r_.load.at[0])] + [
        pltpu.make_async_copy(getattr(r_, f"{name}_h"), getattr(r_, name), r_.load.at[1 + i])
        for i, name in enumerate(("we", "wqkv", "wp", "wo", "wu", "wd", "cot"))
    ]
    own_rows = pltpu.make_async_copy(r_.x_in, r_.gb.at[0, me], r_.load.at[8])
    own_rows.start()
    for load in loads:
        load.start()

    barrier = pltpu.get_barrier_semaphore()
    for dr in range(M):
        for d in range(N):
            if dr + d > 0:
                pl.semaphore_signal(barrier, inc=1, device_id={"rep": (rep + dr) % M, "nodes": (me + d) % N},
                                    device_id_type=MESH)
    pl.semaphore_wait(barrier, M * N - 1)

    def gather_start(l):
        mine = r_.gb.at[l, me]
        send_rows(mine, mine, R, r_.ag_s.at[0], r_.agn_r.at[l], nodes=partner)
        send_rows(mine, mine, R, r_.ag_s.at[0], r_.agn_r.at[l], nodes=2 * z_to(1) + par)
        send_rows(mine, mine, R, r_.ag_s.at[0], r_.agn_r.at[l], nodes=2 * z_to(1) + 1 - par)
        for t in range(2, NZ):
            send_rows(mine, mine, R, r_.ag_s.at[0], r_.agc_r.at[l, t], nodes=2 * z_to(t) + par)

    def gather_pass(l, t):
        piece = r_.gb.at[l, 2 * z_from(t) + par]
        arrive(piece, r_.agc_r.at[l, t])
        send_rows(piece, piece, R, r_.ag_s.at[0], r_.agp_r.at[l], nodes=partner)

    def gather_near(l):
        arrive(r_.gb.at[l, 0:3], r_.agn_r.at[l])

    def gather_far(l):
        arrive(r_.gb.at[l, 0 : NZ - 2], r_.agp_r.at[l])

    def sync_start(k, first, second):
        mine = rep * N + me
        r_.st1[k, mine] = pack(first, second)
        for dr in range(M):
            for d in range(N):
                if dr + d > 0:
                    send(r_.st1.at[k, mine], r_.st1.at[k, mine], r_.st_s.at[0], r_.st_r.at[k],
                         rep=(rep + dr) % M, nodes=(me + d) % N)

    def sync_wait(k):
        arrive(r_.st1.at[k, 0 : M * N - 1], r_.st_r.at[k])

    def sync_moments(k):
        sync_wait(k)
        return unpack(combine_moments(r_.st1[k], float(R)))

    def sync_sums(k):
        sync_wait(k)
        return unpack(jnp.sum(r_.st1[k], 0))

    sizes = axis_sizes(N, M)
    core, row = rep % 2, rep // 2
    places = dict(
        core=(core, lambda t: dict(rep=2 * row + t)),
        y=(row, lambda t: dict(rep=2 * t + core)),
        x=(par, lambda t: dict(nodes=2 * z + t)),
        z=(z, lambda t: dict(nodes=2 * t + par)),
        rep=(rep, lambda t: dict(rep=t)),
        nodes=(me, lambda t: dict(nodes=t)),
    )

    def reduce_step(g, step):
        name, layer, first, rows, stages = GROUPS[g]
        K = len(stages)
        base = sum(2 * len(before) for *_, before in GROUPS[:g])
        gs, out = getattr(r_, f"gs_{name}").at[layer, first : first + rows], getattr(r_, f"go{g}")
        count, offset = [rows], [0]
        for axis in stages:
            count.append(count[-1] // sizes[axis])
            offset.append(offset[-1] + places[axis][0] * count[-1])
        take = lambda start, size: pl.ds(pl.multiple_of(start, 16), size)
        if 1 <= step <= K:
            k = step - 1
            got = getattr(r_, f"ga{g}_{k}")
            arrive(got, r_.ar_r.at[base + k])
            held = gs if k == 0 else getattr(r_, f"gh{g}_{k - 1}")
            index = places[stages[k]][0]
            acc = held[take(index * count[k + 1], count[k + 1])].astype(F32)
            for slot in range(sizes[stages[k]] - 1):
                acc = acc + got[slot].astype(F32)
            if step < K:
                getattr(r_, f"gh{g}_{k}")[...] = acc.astype(BF16)
            else:
                out[take(offset[K], count[K])] = acc.astype(BF16)
        elif step > K:
            k = 2 * K - step
            arrive(out.at[0 : (sizes[stages[k]] - 1) * count[k + 1]], r_.ar_r.at[base + step - 1])
        if step < K:
            held = gs if step == 0 else getattr(r_, f"gh{g}_{step - 1}")
            index, device = places[stages[step]]
            size = sizes[stages[step]]
            for d in range(1, size):
                to = (index + d) % size
                send_rows(held.at[take(to * count[step + 1], count[step + 1])], getattr(r_, f"ga{g}_{step}").at[d - 1],
                     count[step + 1], r_.ar_s.at[g], r_.ar_r.at[base + step], **device(to))
        elif step < 2 * K:
            k = 2 * K - 1 - step
            index, device = places[stages[k]]
            size = sizes[stages[k]]
            here = out.at[take(offset[k + 1], count[k + 1])]
            for d in range(1, size):
                send_rows(here, here, count[k + 1], r_.ar_s.at[g], r_.ar_r.at[base + step],
                          **device((index + d) % size))
        else:
            pltpu.make_async_copy(out, getattr(r_, f"gout{g}"), r_.ar_l.at[g]).start()

    def reduce_drain(g):
        name, _, _, rows, _ = GROUPS[g]
        sent(getattr(r_, f"gs_{name}").at[:, 0 : rows - rows // (M * N)], r_.ar_s.at[g])
        pltpu.make_async_copy(getattr(r_, f"go{g}"), getattr(r_, f"gout{g}"), r_.ar_l.at[g]).wait()

    def put(buf, l, at, value):
        rows = value.shape[0]
        for c in range(value.shape[1] // 128):
            buf[l, at : at + rows] = value[:, 128 * c : 128 * (c + 1)].astype(BF16)
            at += rows
        return at

    lane_head = lax.broadcasted_iota(I32, (R, 128), 1) // HEAD_DIM

    def by_head(parts):
        out = parts[0]
        for k in range(1, HK):
            out = jnp.where(lane_head == k, parts[k], out)
        return out

    r_.meta[me] = jnp.full((8, 256), -1, I32)
    r_.meta[me, 0:1, 0:R] = r_.ids[...].reshape(1, R)
    r_.meta[me, 1:2, 0:48] = r_.halo[...].reshape(1, 48)
    for d in range(1, N):
        send(r_.meta.at[me], r_.meta.at[me], r_.meta_s.at[0], r_.meta_r.at[0], nodes=(me + d) % N)
    own_rows.wait()
    gather_start(0)

    src_row = r_.edge_src[...].reshape(1, E)
    src_row = jnp.where(src_row < R + 24, src_row, src_row + 8)
    dst_row = r_.edge_dst[...].reshape(1, E)
    src_col = jnp.broadcast_to(src_row, (128, E)).T[:, 0:1]
    dst_col = jnp.broadcast_to(dst_row, (128, E)).T[:, 0:1]
    as_mask = lambda cond: cond.astype(F32).astype(BF16)
    r_.le[:, 0:256] = as_mask(src_col == lax.broadcasted_iota(I32, (E, 256), 1))
    target = as_mask(dst_col == lax.broadcasted_iota(I32, (E, 256), 1))
    r_.le[:, 512:768] = target
    r_.le[:, 768:1024] = target
    target = as_mask(dst_row == lax.broadcasted_iota(I32, (R, E), 0))
    r_.TT[:, 0:E] = target
    r_.TT[:, E:] = target
    r_.ST[...] = as_mask(src_row == lax.broadcasted_iota(I32, (256, E), 0))
    r_.dn[R:256] = jnp.zeros((256 - R, 2 * D), BF16)
    r_.dn[256 + R : 512] = jnp.zeros((256 - R, 2 * D), BF16)
    r_.dproj[R:256, 0:D] = jnp.zeros((256 - R, D), BF16)
    r_.dproj[R:256, 2 * D : 3 * D] = jnp.zeros((256 - R, D), BF16)
    loads[0].wait()
    r_.efT[...] = r_.le[:, D : 2 * D].T
    for l in range(L):
        for k in range(3):
            r_.gain[l, k : k + 1] = r_.gain_in[k, l : l + 1]
            r_.shift[l, k : k + 1] = r_.shift_in[k, l : l + 1]
    r_.xf[0] = r_.gb[0, me].astype(F32)
    r_.moff[...] = jnp.zeros((N, 8, D), F32)
    r_.move[0:1] = jnp.ones((1, D), F32)
    r_.move[1:2] = jnp.zeros((1, D), F32)
    for load in loads[1:]:
        load.wait()
    for l in range(L):
        r_.wkvT[l] = r_.wqkv[l, :, D:].T

    arrive(r_.meta.at[0 : N - 1], r_.meta_r.at[0])
    id_col = jnp.broadcast_to(r_.meta[me][0:1, 0:R], (128, R)).T[:, 0:1]
    id_row = jnp.concatenate(
        [r_.meta[4 * ((zh + NB - j // 4) % NB) + j % 4][0:1, 0:R] for j in range(N)], 1
    )
    r_.bias[...] = jnp.where(id_col == id_row, 0.0, NEG)

    def halo_onehot(device, start):
        col = jnp.broadcast_to(r_.meta[device][1:2, 0:128], (128, 128)).T[start : start + 24, 0:1]
        hot = (col == lax.broadcasted_iota(I32, (24, R), 1)).astype(F32)
        return jnp.concatenate([hot, jnp.zeros((8, R), F32)], 0).astype(BF16)

    r_.HP[...] = halo_onehot(prev, 24)
    r_.HN[...] = halo_onehot(nxt, 0)
    r_.A[...] = as_mask(r_.meta[me][1:2, 0:64] == lax.broadcasted_iota(I32, (R, 64), 0))

    factor_exp = scale * math.log2(math.e)

    def prepare_queries(l):
        q = dot(r_.xs[l, me], r_.wqkv[l, :, :D]).astype(BF16)
        r_.q[l] = q
        q = q.astype(F32)
        for hf in range(2):
            for k in range(HK):
                part = jnp.where(lane_head == k, q[:, 128 * hf : 128 * (hf + 1)], 0.0)
                r_.qm[l, hf, k * R : (k + 1) * R] = part.astype(BF16)

    def head_dims(hf, k, base=0):
        first = base + hf * 128 + k * HEAD_DIM
        return slice(first, first + HEAD_DIM)

    def head_rows(hf, k, count=1):
        return slice((hf * HK + k) * R, (hf * HK + k + count) * R)

    def lane_half(hf):
        return slice(hf * 128, (hf + 1) * 128)

    def half_of(i):
        return (zh + NB - i) % NB, slice(i * W, (i + 1) * W)

    def attention_keys(l, i):
        half, rows = half_of(i)
        x = r_.xs[l, pl.ds(4 * half, 4)].reshape(W, D)
        r_.kvT[l, :, rows] = dot_nt(r_.wkvT[l], x).astype(BF16)

    def attention_heads(l, i, hfs):
        _, rows = half_of(i)
        for hf in hfs:
            lanes = lane_half(hf)
            ones = jnp.ones((HEAD_DIM, W), BF16)
            for c in range(HK // 2):
                r_.sc[c % 2, 0 : 2 * R] = dot(r_.qm[l, hf, 2 * c * R : 2 * (c + 1) * R], r_.kvT[l, lanes, rows])
                for k in range(2):
                    for at in range(0, R, STRIP):
                        s = r_.sc[c % 2, k * R + at : k * R + at + STRIP] + r_.bias[at : at + STRIP, rows]
                        top = jnp.max(s, 1, keepdims=True)
                        e = jnp.exp2((s - top) * factor_exp)
                        r_.tp[2 * c + k, at : at + STRIP] = jnp.broadcast_to(top, (STRIP, 128))
                        first = (hf * HK + 2 * c + k) * R + at
                        r_.pst[l, first : first + STRIP, rows] = e.astype(BF16)
                for k in range(2):
                    h = 2 * c + k
                    left = jnp.concatenate([r_.kvT[l, head_dims(hf, h, D), rows], ones], 0)
                    o = dot_nt(left, r_.pst[l, head_rows(hf, h), rows])
                    r_.odT[i, head_dims(hf, h)] = o[0:HEAD_DIM]
                    r_.ldT[i, head_dims(hf, h)] = o[HEAD_DIM:]
            r_.md[i, :, lanes] = by_head([r_.tp[k] for k in range(HK)])

    def attention_end(l):
        tops = [r_.md[i].T for i in range(NB)]
        top = tops[0]
        for i in range(1, NB):
            top = jnp.maximum(top, tops[i])
        factors = [jnp.exp2((tops[i] - top) * factor_exp) for i in range(NB)]
        inv = 1.0 / sum(factors[i] * r_.ldT[i] for i in range(NB))
        o = jnp.zeros((D, R), F32)
        for i in range(NB):
            r_.rb[l, i] = (factors[i] * inv).T
            o = o + factors[i] * inv * r_.odT[i]
        o = o.T
        r_.oraw[l] = o
        ob = o.astype(BF16)
        r_.ob[l] = ob
        t1 = r_.xf[l] + dot(ob, r_.wo[l])
        r_.z1[l] = t1
        mean1 = col_sum(t1) / R
        return mean1, col_sum((t1 - mean1) * (t1 - mean1))

    def convolution(l):
        xs = r_.xs
        xb = xs[l, me]
        r_.xe[l, 0:R] = xb
        r_.xe[l, R : R + 32] = dot(r_.HP[...], xs[l, prev]).astype(BF16)
        r_.xe[l, R + 32 : R + 64] = dot(r_.HN[...], xs[l, nxt]).astype(BF16)
        xe = r_.xe[l]
        made = dot(xe, r_.wp[l])
        pd_high, pd_low = split(made[:, 2 * D : 3 * D])
        r_.re[0:256] = made[:, 3 * D :].astype(BF16)
        r_.re[256:512] = r_.we[l]
        r_.re[512:768] = pd_high
        r_.re[768:1024] = pd_low
        r_.gate[l] = dot(r_.le[...], r_.re[...])
        r_.bs[l] = dot(r_.le[:, 0:256], made[:, D : 2 * D].astype(BF16)).astype(BF16)
        for at in range(0, E, 64):
            here = slice(at, at + 64)
            gate = sigmoid(r_.gate[l, here])
            r_.gate[l, here] = gate
            high, low = split(jnp.concatenate([gate * r_.bs[l, here].astype(F32), gate], 1))
            r_.gg[here] = high
            r_.gg[E + at : E + at + 64] = low
        num_den = dot(r_.TT[...], r_.gg[...])
        pa, num, den = made[0:R, 0:D], num_den[:, 0:D], num_den[:, D:]
        r_.num[l] = num
        r_.den[l] = den
        msg = pa + num / (den + GATE_EPS)
        r_.z0[l] = msg
        mean0 = col_sum(msg) / R
        return mean0, col_sum((msg - mean0) * (msg - mean0))

    def forward(l):
        def ready(js):
            for j in js:
                moved = (r_.gb[l, j].astype(F32) + r_.moff[j, 0:1]) * r_.move[0:1] + r_.move[1:2]
                r_.xs[l, j] = moved.astype(BF16)

        r_.xs[l, me] = r_.xf[l].astype(BF16)
        prepare_queries(l)
        gather_near(l)
        ready([partner, 2 * z_from(1) + par, 2 * z_from(1) + 1 - par])

        attention_keys(l, 0)
        attention_heads(l, 0, (0,))
        for t in range(2, NZ):
            gather_pass(l, t)
        attention_heads(l, 0, (1,))
        gather_far(l)
        ready([2 * z_from(t) + p for t in range(2, NZ) for p in range(2)])
        mean0, sq0 = convolution(l)
        for i in range(1, NB):
            attention_keys(l, i)
            attention_heads(l, i, (0, 1))
        sync_start(3 * l, mean0, sq0)
        mean1, sq1 = attention_end(l)
        sync_start(3 * l + 1, mean1, sq1)
        mean0, sq0 = sync_moments(3 * l)
        inv0 = lax.rsqrt(sq0 / total + NORM_EPS)
        r_.iv[l, 0:1] = inv0
        z0 = (r_.z0[l] - mean0) * inv0
        r_.z0[l] = z0
        n0 = z0 * r_.gain[l, 0:1] + r_.shift[l, 0:1]
        r_.local[...] = r_.xf[l] + n0 * sigmoid(n0)
        mean1, sq1 = sync_moments(3 * l + 1)
        inv1 = lax.rsqrt(sq1 / total + NORM_EPS)
        r_.iv[l, 1:2] = inv1
        z1 = (r_.z1[l] - mean1) * inv1
        r_.z1[l] = z1
        mix = r_.local[...] + z1 * r_.gain[l, 1:2] + r_.shift[l, 1:2]
        mb = mix.astype(BF16)
        r_.mb[l] = mb
        u = dot(mb, r_.wu[l])
        r_.u[l] = u
        g = (u * sigmoid(u)).astype(BF16)
        r_.g[l] = g
        y = mix + dot(g, r_.wd[l])
        r_.z2[l] = y
        mean = col_sum(y) / R
        cent = y - mean
        k = 3 * l + 2
        sync_start(k, mean, col_sum(cent * cent))

        if l < L - 1:
            r_.gb[l + 1, me] = cent.astype(BF16)
            gather_start(l + 1)

        if l == L - 1:
            dy = r_.cot[...].astype(F32)
            sync_start(3 * L, col_sum(dy), col_sum(dy * cent))

        tot_mean, tot_sq = sync_moments(k)
        inv2 = lax.rsqrt(tot_sq / total + NORM_EPS)
        r_.iv[l, 2:3] = inv2
        z2 = (r_.z2[l] - tot_mean) * inv2
        r_.z2[l] = z2
        gain, shift = r_.gain[l, 2:3], r_.shift[l, 2:3]
        r_.xf[l + 1] = z2 * gain + shift

        if l == L - 1:
            sync_wait(3 * L)
            sums, means = r_.st1[3 * L], r_.st1[k][:, 0:2]
            mean = jnp.mean(means, 0)
            dy_sum = jnp.sum(sums[:, 0:2], 0)
            dy_cent = jnp.sum(sums[:, 2:4] + (means - mean) * sums[:, 0:2], 0)
            dy_sum, dy_cent = unpack(jnp.concatenate([dy_sum, dy_cent], 0))
            r_.gshift[l, 2:3] = dy_sum
            r_.ggain[l, 2:3] = dy_cent * inv2

        for j in range(N):
            tile = r_.st1[k, rep * N + j]
            r_.moff[j, 0:1] = jnp.concatenate([tile[0:1], tile[1:2]], 1) - tot_mean
        r_.move[0:1] = inv2 * gain
        r_.move[1:2] = shift

    for l in range(L):
        forward(l)
    act_copy = pltpu.make_async_copy(r_.xf.at[L], r_.out_act, r_.store.at[0])
    act_copy.start()

    def back_feed_forward(l, k):
        s2, g2 = r_.gshift[l, 2:3], r_.ggain[l, 2:3]
        d3 = r_.gain[l, 2:3] * r_.iv[l, 2:3] * (r_.dy[...] - s2 / total - r_.z2[l] * (g2 / total))
        db = d3.astype(BF16)
        dub = (dot_nt(db, r_.wd[l]) * silu_slope(r_.u[l])).astype(BF16)
        dmix = d3 + dot_nt(dub, r_.wu[l])
        r_.dmix[...] = dmix
        n0 = r_.z0[l] * r_.gain[l, 0:1] + r_.shift[l, 0:1]
        gy0 = dmix * silu_slope(n0)
        sync_start(k, col_sum(dmix), col_sum(dmix * r_.z1[l]))
        sync_start(k + 1, col_sum(gy0), col_sum(gy0 * r_.z0[l]))
        r_.gy0[...] = gy0
        at = put(r_.gs_early, l, 512, dot_tn(r_.mb[l], dub))
        put(r_.gs_early, l, at, dot_tn(r_.g[l], db))
        r_.xeT[...] = r_.xe[l].T
        r_.qT[...] = r_.q[l].T

    def back_norms(l, k):
        s1, g1 = sync_sums(k)
        r_.gshift[l, 1:2] = s1
        r_.ggain[l, 1:2] = g1
        dmix = r_.dmix[...]
        d2 = r_.gain[l, 1:2] * r_.iv[l, 1:2] * (dmix - s1 / total - r_.z1[l] * (g1 / total))
        dab = d2.astype(BF16)
        r_.dxo[...] = dmix + d2
        r_.dob[...] = dot_nt(dab, r_.wo[l]).astype(BF16).astype(F32)
        put(r_.gs_early, l, 0, dot_tn(r_.ob[l], dab))
        r_.gkv[...] = jnp.zeros((2 * D, D), F32)
        r_.dqT[...] = jnp.zeros((D, R), F32)

    def back_half(i):
        t1 = (i + 1) % NB
        half = (zh + t1) % NB
        place = (NB - t1) % NB
        return place, half, slice(place * W, (place + 1) * W)

    def back_heads(l, i, hf):
        place, half, rows = back_half(i)
        if True:
            lanes = lane_half(hf)
            dos = r_.dob[:, lanes] * r_.rb[l, place, :, lanes]
            prod = dos * r_.oraw[l, :, lanes]
            for k in range(HK):
                r_.dom[k * R : (k + 1) * R, 0:128] = jnp.where(lane_head == k, dos, 0.0).astype(BF16)
                r_.dom[k * R : (k + 1) * R, 128:256] = jnp.where(lane_head == k, -prod, 0.0).astype(BF16)
            r_.dosT[...] = dos.T.astype(BF16)
            values = slice(D + hf * 128, D + (hf + 1) * 128)
            right = jnp.concatenate([r_.kvT[l, values, rows], jnp.ones((128, W), BF16)], 0)
            for c in range(HK // 2):
                both = slice(2 * c * R, 2 * (c + 1) * R)
                r_.sc[c % 2, 0 : 2 * R] = dot(r_.dom[both], right)
                for k in range(2):
                    for at in range(0, R, STRIP):
                        first = (hf * HK + 2 * c + k) * R + at
                        e = r_.pst[l, first : first + STRIP, rows].astype(F32)
                        ds = e * r_.sc[c % 2, k * R + at : k * R + at + STRIP]
                        r_.dss[(2 * c + k) * R + at : (2 * c + k) * R + at + STRIP] = ds.astype(BF16)
                for k in range(2):
                    h = 2 * c + k
                    mine, dims = slice(h * R, (h + 1) * R), head_dims(hf, h)
                    r_.dqT[dims] += dot_nt(r_.kvT[l, dims, rows], r_.dss[mine])
                    r_.dkv[dims] = (dot(r_.qT[dims], r_.dss[mine]) * scale).astype(BF16)
                    dv = dot(r_.dosT[h * HEAD_DIM : (h + 1) * HEAD_DIM], r_.pst[l, head_rows(hf, h), rows])
                    r_.dkv[head_dims(hf, h, D)] = dv.astype(BF16)

    def back_rows(l, i):
        _, half, _ = back_half(i)
        dx = dot(r_.wqkv[l, :, D:], r_.dkv[...]).T
        r_.dxs[l, pl.ds(2 * half, 2)] = dx.astype(BF16).reshape(2, 2, R, D)

        if i < NB - 1:
            for low in range(2):
                zb = 2 * half + low
                send_rows(r_.dxs.at[l, zb, 1 - par], r_.rs1.at[l, zb], R,
                     r_.rs_s.at[0], r_.rsp_r.at[l, i], nodes=partner)

        else:
            near = z_to(1)
            send_rows(r_.dxs.at[l, z, 1 - par], r_.ro.at[l, 0], R, r_.rs_s.at[0], r_.ro_r.at[l], nodes=partner)
            send_rows(r_.dxs.at[l, near, par], r_.ro.at[l, 1], R, r_.rs_s.at[0], r_.ro_r.at[l], nodes=2 * near + par)
            send_rows(r_.dxs.at[l, near, 1 - par], r_.ro.at[l, 2], R, r_.rs_s.at[0], r_.ro_r.at[l],
                 nodes=2 * near + 1 - par)

        r_.gkv[...] += dot(r_.dkv[...], r_.xs[l, pl.ds(4 * half, 4)].reshape(W, D))

    def pass_on(l, i, t):
        zb = z_to(t)
        if t % 2 == 0:
            arrive(r_.rs1.at[l, 0:2], r_.rsp_r.at[l, i])
        both = r_.dxs[l, zb, par].astype(F32) + r_.rs1[l, zb].astype(F32)
        r_.cs[l, zb] = both.astype(BF16)
        send_rows(r_.cs.at[l, zb], r_.rs2.at[l, z], R, r_.rs_s.at[0], r_.rsc_r.at[l], nodes=2 * zb + par)

    def back_convolution(l, k):
        s0, g0 = unpack(jnp.sum(r_.st1[k + 1], 0))
        r_.gshift[l, 0:1] = s0
        r_.ggain[l, 0:1] = g0
        inv_den = 1.0 / (r_.den[l] + GATE_EPS)
        dm = r_.gain[l, 0:1] * r_.iv[l, 0:1] * (r_.gy0[...] - s0 / total - r_.z0[l] * (g0 / total))
        dnum = dm * inv_den
        dden = -dnum * r_.num[l] * inv_den
        high, low = split(jnp.concatenate([dnum, dden], 1))
        r_.dn[0:R] = high
        r_.dn[256 : 256 + R] = low
        r_.sc[0, 0:E, 0 : 2 * D] = dot(r_.le[:, 512:1024], r_.dn[...])
        for at in range(0, E, 64):
            here = slice(at, at + 64)
            gate, dnum_e = r_.gate[l, here], r_.sc[0, here, 0:D]
            dgp = (dnum_e * r_.bs[l, here].astype(F32) + r_.sc[0, here, D : 2 * D]) * gate * (1.0 - gate)
            r_.gg[here, 0:D] = (dnum_e * gate).astype(BF16)
            r_.gg[here, D:] = dgp.astype(BF16)
        ext = dot(r_.ST[...], r_.gg[0:E]).astype(BF16)
        r_.dproj[0:R, 0:D] = dm.astype(BF16)
        r_.dproj[:, D : 2 * D] = ext[:, 0:D]
        r_.dproj[0:R, 2 * D : 3 * D] = dot(r_.TT[:, 0:E], r_.gg[0:E, D:]).astype(BF16)
        r_.dproj[:, 3 * D :] = ext[:, D:]
        dxe = dot_nt(r_.dproj[...], r_.wp[l])
        r_.hs[l, 0] = dxe[R : R + 32].astype(BF16)
        r_.hs[l, 1] = dxe[R + 32 : R + 64].astype(BF16)
        r_.dxo[...] += dxe[0:R]

    def send_halo(l):
        send(r_.hs.at[l, 0], r_.hr.at[l, 1], r_.hal_s.at[0], r_.hal_r.at[l], nodes=prev)
        send(r_.hs.at[l, 1], r_.hr.at[l, 0], r_.hal_s.at[0], r_.hal_r.at[l], nodes=nxt)

    def conv_weight_grads(l):
        at = put(r_.gs_conv, l, 0, dot(r_.xeT[...], r_.dproj[...]))
        put(r_.gs_conv, l, at, dot(r_.efT[...], r_.gg[0:E, D:]))

    def back_input(l):
        dx = r_.dxo[...]
        dx = dx + r_.dxs[l, z, par].astype(F32)
        arrive(r_.ro.at[l], r_.ro_r.at[l])
        for slot in range(3):
            dx = dx + r_.ro[l, slot].astype(F32)
        if NZ > 2:
            arrive(r_.rs2.at[l, 0 : NZ - 2], r_.rsc_r.at[l])
        for t in range(2, NZ):
            dx = dx + r_.rs2[l, z_from(t)].astype(F32)
        arrive(r_.hr.at[l], r_.hal_r.at[l])
        back = jnp.concatenate(
            [r_.hr[l, 0].astype(F32)[0:24], r_.hr[l, 1].astype(F32)[0:24], jnp.zeros((16, D), F32)], 0
        )
        return dx + dot(r_.A[...], back.astype(BF16))

    r_.dy[...] = r_.cot[...].astype(F32)

    E1, C1, Q1, E0, C0, QK0, V0 = range(len(GROUPS))

    def steps(*pairs):
        return [functools.partial(reduce_step, g, k) for g, k in pairs]

    r_.dy[...] = r_.cot[...].astype(F32)

    def backward(b):
        l = L - 1 - b
        first, last = b == 0, b == L - 1
        k = 3 * L + 1 + 2 * b
        back_feed_forward(l, k)
        when(last, *steps((C1, 4), (Q1, 2), (E1, 6)))
        back_norms(l, k)
        sync_wait(k + 1)
        when(first, *steps((E1, 0)))
        when(last, *steps((C1, 5), (Q1, 3), (E0, 0)))
        back_convolution(l, k)
        back_heads(l, 0, 0)
        send_halo(l)
        when(first, *steps((E1, 1)))
        when(last, *steps((C1, 6), (Q1, 4), (E0, 1)))
        conv_weight_grads(l)
        back_heads(l, 0, 1)
        back_rows(l, 0)
        when(first, *steps((C1, 0), (E1, 2)))
        when(last, *steps((C0, 0), (E0, 2), (C1, 7), (Q1, 5)))
        back_heads(l, 1, 0)
        for t in range(2, NZ):
            pass_on(l, 0, t)
        when(first, *steps((C1, 1), (E1, 3)))
        when(last, *steps((C0, 1), (E0, 3), (C1, 8), (Q1, 6)))
        back_heads(l, 1, 1)
        back_rows(l, 1)
        when(first, *steps((C1, 2), (E1, 4)))
        when(last, *steps((C0, 2), (E0, 4)))
        dqb = (r_.dqT[...].T * scale).astype(BF16)
        r_.dxo[...] += dot_nt(dqb, r_.wqkv[l, :, 0:D])
        at = put(r_.gs_qkv, l, 0, dot(r_.xeT[:, 0:R], dqb))
        put(r_.gs_qkv, l, at, r_.gkv[...].T)
        when(first, *steps((Q1, 0)))

        if first:
            dx = back_input(l)
            r_.dy[...] = dx
            below = L - 2
            sync_start(SYNCS - 1, col_sum(dx), col_sum(dx * r_.z2[below]))
            for step in steps((C1, 3), (Q1, 1), (E1, 5)):
                step()
            s2, g2 = sync_sums(SYNCS - 1)
            r_.gshift[below, 2:3] = s2
            r_.ggain[below, 2:3] = g2


    for b in range(L):
        backward(b)
    for step in steps((QK0, 0), (V0, 0), (E0, 5), (C0, 3), (V0, 1), (QK0, 1)):
        step()
    r_.dy[...] = back_input(0)
    in_copy = pltpu.make_async_copy(r_.dy, r_.grad_in, r_.store.at[1])
    in_copy.start()
    for step in steps(
        (E0, 6), (C0, 4), (V0, 2), (QK0, 2),
        (E0, 7), (C0, 5), (V0, 3), (QK0, 3),
        (E0, 8), (C0, 6), (V0, 4), (QK0, 4),
    ):
        step()
    for l in range(L):
        for k in range(3):
            r_.ggain_out[k, l : l + 1] = r_.ggain[l, k : k + 1]
            r_.gshift_out[k, l : l + 1] = r_.gshift[l, k : k + 1]
    for g in range(len(GROUPS)):
        reduce_drain(g)
    sent(r_.meta.at[0 : N - 1], r_.meta_s.at[0])
    sent(r_.st1.at[:, 0 : M * N - 1], r_.st_s.at[0])
    sent(r_.gb.at[:, 0 : 3 + 2 * (NZ - 2)], r_.ag_s.at[0])
    sent(r_.gb.at[:, 0 : 2 * (NB - 1) + 3 + NZ - 2], r_.rs_s.at[0])
    sent(r_.hs, r_.hal_s.at[0])
    act_copy.wait()
    in_copy.wait()


def finish_kernel(act_h, gin_h, *refs):
    n = len(GROUPS)
    held, (ggain_h, gshift_h), refs = refs[:n], refs[n : n + 2], refs[n + 2 :]
    act_o, gin_o, proj_o, edge_o, qkv_o, out_o, up_o, down_o, ggain_o, gshift_o = refs[:10]
    summed, refs = refs[10 : 10 + n], refs[10 + n :]
    act, gin, proj, edge, qkv, out, up, down, in_sem, out_sem = refs
    loads = [
        pltpu.make_async_copy(src, dst, in_sem.at[i])
        for i, (src, dst) in enumerate(zip(held + (act_h, gin_h), summed + (act, gin), strict=True))
    ]
    for load in loads:
        load.start()
    ggain_o[...] = ggain_h[...]
    gshift_o[...] = gshift_h[...]
    stores = []

    def store(src, dst):
        copy = pltpu.make_async_copy(src, dst, out_sem.at[len(stores)])
        copy.start()
        stores.append(copy)

    def widen(dst, l, g, at, first=0, last=None):
        rows = dst.shape[1]
        for c in range(first, dst.shape[2] // 128 if last is None else last):
            dst[l, :, 128 * c : 128 * (c + 1)] = summed[g][at : at + rows].astype(F32)
            at += rows
        return at

    for g, (name, l, first, rows, _) in enumerate(GROUPS):
        loads[g].wait()
        if name == "early":
            at = widen(out, l, g, 0)
            store(out.at[l], out_o.at[l])
            at = widen(up, l, g, at)
            store(up.at[l], up_o.at[l])
            widen(down, l, g, at)
            store(down.at[l], down_o.at[l])
        elif name == "conv":
            at = widen(proj, l, g, 0)
            store(proj.at[l], proj_o.at[l])
            widen(edge, l, g, at)
            store(edge.at[l], edge_o.at[l])
        else:
            widen(qkv, l, g, 0, first // 256, (first + rows) // 256)
            if first + rows == 1536:
                store(qkv.at[l], qkv_o.at[l])
    for i, (src, dst) in enumerate(((act, act_o), (gin, gin_o))):
        loads[n + i].wait()
        store(src, dst)
    for copy in stores:
        copy.wait()


def fused_device(
    N, M, node_input, edge_feat, graph_ids, edge_src, edge_dst, halo_send, w_proj, w_edge, w_qkv,
    w_out, w_up, w_down, norm_gain, norm_shift, cotangent,
):
    R, D = node_input.shape
    E = edge_feat.shape[0]
    L = w_proj.shape[0]
    names = scratch_list(N, M, L, R, E)
    vmem = pl.BlockSpec(memory_space=pltpu.VMEM)
    hbm = pl.BlockSpec(memory_space=pltpu.HBM)
    shape = jax.ShapeDtypeStruct
    rows = shape((R, D), F32)
    norm = shape((3, L, D), F32)
    groups = [shape((rows_g, 128), BF16) for _, _, _, rows_g, _ in GROUPS]
    outs = pl.pallas_call(
        functools.partial(kernel, N, M, L, tuple(names)),
        out_shape=[rows, rows, *groups, norm, norm],
        in_specs=[hbm] + [vmem] * 4 + [hbm] * 7 + [vmem] * 2 + [hbm],
        out_specs=[hbm] * (2 + len(GROUPS)) + [vmem] * 2,
        scratch_shapes=list(names.values()),
        compiler_params=pltpu.CompilerParams(
            collective_id=0, has_side_effects=True, vmem_limit_bytes=60 << 20
        ),
        name="layers",
    )(node_input, graph_ids, edge_src, edge_dst, halo_send, edge_feat, w_proj, w_edge, w_qkv, w_out, w_up,
      w_down, norm_gain.transpose(1, 0, 2), norm_shift.transpose(1, 0, 2), cotangent)
    weights = [shape(w.shape, F32) for w in (w_proj, w_edge, w_qkv, w_out, w_up, w_down)]
    results = pl.pallas_call(
        finish_kernel,
        out_shape=[rows, rows, *weights, norm, norm],
        in_specs=[hbm] * (2 + len(GROUPS)) + [vmem] * 2,
        out_specs=[hbm] * 8 + [vmem] * 2,
        scratch_shapes=[pltpu.VMEM(s.shape, s.dtype) for s in (*groups, rows, rows, *weights)]
        + [pltpu.SemaphoreType.DMA((len(GROUPS) + 2,)), pltpu.SemaphoreType.DMA((14,))],
        compiler_params=pltpu.CompilerParams(vmem_limit_bytes=60 << 20),
        name="gradients",
    )(*outs)
    ggain, gshift = results[8].transpose(1, 0, 2), results[9].transpose(1, 0, 2)
    return (*results[:8], ggain, gshift)


BLOCK_CAP = 2048


def extended_2(block, sides, width):
    for axis, dim in sides:
        count = lax.axis_size(axis)
        forward = [(i, i + 1) for i in range(count - 1)]
        forward.append((count - 1, 0))
        backward = [(target, source) for source, target in forward]
        low = lax.ppermute(
            lax.slice_in_dim(block, block.shape[dim] - width, None, axis=dim), axis, forward
        )
        high = lax.ppermute(lax.slice_in_dim(block, 0, width, axis=dim), axis, backward)
        block = jnp.concatenate([low, block, high], axis=dim)
    return block


def block_length(total_rows, upper_limit):
    for length in range(min(total_rows, upper_limit), 0, -1):
        if total_rows % length == 0:
            return length
    return 1


def outer_product(left, right):
    return lax.dot_general(
        left, right, (((0,), (0,)), ((), ())), preferred_element_type=jnp.float32
    )


def times_transposed(left, weight):
    return lax.dot_general(
        left, weight, (((1,), (1,)), ((), ())), preferred_element_type=jnp.float32
    )


def forward_product(left, weight):
    return jnp.dot(left, weight, preferred_element_type=jnp.float32)


def silu_slope_plain(inputs):
    logistic = jax.nn.sigmoid(inputs)
    return logistic * (1.0 + inputs * (1.0 - logistic))


def normalize(inputs, gain_row, shift_row, node_total):
    batch_mean = lax.psum(jnp.sum(inputs, 0), ("nodes", "rep")) / node_total
    centred = inputs - batch_mean
    batch_var = lax.psum(jnp.sum(centred * centred, 0), ("nodes", "rep")) / node_total
    inv_std = lax.rsqrt(batch_var + NORM_EPS)
    standard = (inputs - batch_mean) * inv_std
    return (standard * gain_row + shift_row, standard, inv_std)


def normalize_back(grad_out, standard, inv_std, gain_row, node_total):
    shift_grad, gain_grad = lax.psum(
        (jnp.sum(grad_out, 0), jnp.sum(grad_out * standard, 0)), ("nodes", "rep")
    )
    grad_in = (
        gain_row
        * inv_std
        * (grad_out - shift_grad / node_total - standard * gain_grad / node_total)
    )
    return (grad_in, gain_grad, shift_grad)


def exchange_sources(outgoing):
    halo_rows = outgoing.shape[0] // 2
    grown = extended_2(outgoing, (("nodes", 0),), halo_rows)
    return jnp.concatenate([grown[:halo_rows], grown[3 * halo_rows :]], 0)


def return_sources(incoming_grad):
    halo_rows = incoming_grad.shape[0] // 2
    grown = extended_2(incoming_grad.astype(jnp.bfloat16), (("nodes", 0),), halo_rows).astype(
        incoming_grad.dtype
    )
    return jnp.concatenate([grown[:halo_rows], grown[3 * halo_rows :]], 0)


def attend_forward(query_rows, key_rows, value_rows, local_graphs, group_graphs):
    row_count = query_rows.shape[0]
    score_scale = HEAD_DIM ** (-0.5)
    queries = query_rows.reshape(row_count, HEADS, HEAD_DIM)

    def add_piece(carried, kv_piece, first_row):
        key_piece, value_piece = kv_piece
        piece_rows = key_piece.shape[0]
        block_len = block_length(piece_rows, BLOCK_CAP)

        def add_block(block_state, block_index):
            row_max, row_sum, accumulated = block_state
            block_start = block_index * block_len
            key_block = lax.dynamic_slice_in_dim(key_piece, block_start, block_len, 0).reshape(
                block_len, HEADS, HEAD_DIM
            )
            value_block = lax.dynamic_slice_in_dim(value_piece, block_start, block_len, 0).reshape(
                block_len, HEADS, HEAD_DIM
            )
            key_graphs = lax.dynamic_slice_in_dim(
                group_graphs, first_row + block_start, block_len, 0
            )
            same_graph = (local_graphs[:, None] == key_graphs[None, :])[None]
            scores = (
                jnp.einsum("qhd,khd->hqk", queries, key_block, preferred_element_type=jnp.float32)
                * score_scale
            )
            scores = jnp.where(same_graph, scores, NEG)
            new_max = jnp.maximum(row_max, jnp.max(scores, 2))
            weights = jnp.where(same_graph, jnp.exp(scores - new_max[:, :, None]), 0.0)
            factor = jnp.exp(row_max - new_max)
            row_sum = row_sum * factor + jnp.sum(weights, 2)
            contrib = jnp.einsum(
                "hqk,khd->qhd",
                weights.astype(jnp.bfloat16),
                value_block,
                preferred_element_type=jnp.float32,
            )
            accumulated = accumulated * jnp.transpose(factor)[:, :, None] + contrib
            return ((new_max, row_sum, accumulated), None)

        carried, _ = lax.scan(add_block, carried, jnp.arange(piece_rows // block_len))
        return carried

    start_state = (
        jnp.full((HEADS, row_count), NEG, jnp.float32),
        jnp.zeros((HEADS, row_count), jnp.float32),
        jnp.zeros((row_count, HEADS, HEAD_DIM), jnp.float32),
    )
    row_max, row_sum, accumulated = add_piece(
        start_state,
        (
            lax.all_gather(key_rows, "nodes", axis=0, tiled=True),
            lax.all_gather(value_rows, "nodes", axis=0, tiled=True),
        ),
        jnp.int32(0),
    )
    attn_raw = accumulated / jnp.transpose(row_sum)[:, :, None]
    log_sum = row_max + jnp.log(row_sum)
    return (attn_raw, log_sum)


def attend_backward(
    query_rows, key_rows, value_rows, grad_low, attn_raw, log_sum, local_graphs, group_graphs
):
    row_count = query_rows.shape[0]
    model_width = HEADS * HEAD_DIM
    score_scale = HEAD_DIM ** (-0.5)
    queries = query_rows.reshape(row_count, HEADS, HEAD_DIM)
    grad_heads = grad_low.reshape(row_count, HEADS, HEAD_DIM)
    row_delta = jnp.einsum("qhd,qhd->hq", grad_heads.astype(jnp.float32), attn_raw)

    def score_block(key_block, value_block, key_graphs):
        same_graph = (local_graphs[:, None] == key_graphs[None, :])[None]
        scores = (
            jnp.einsum("qhd,khd->hqk", queries, key_block, preferred_element_type=jnp.float32)
            * score_scale
        )
        attn_weights = jnp.exp(jnp.where(same_graph, scores - log_sum[:, :, None], NEG))
        grad_weights = jnp.einsum(
            "qhd,khd->hqk", grad_heads, value_block, preferred_element_type=jnp.float32
        )
        grad_scores = (attn_weights * (grad_weights - row_delta[:, :, None])).astype(jnp.bfloat16)
        return (attn_weights, grad_scores)

    def key_terms(attn_weights, grad_scores, block_len):
        grad_keys = (
            jnp.einsum("hqk,qhd->khd", grad_scores, queries, preferred_element_type=jnp.float32)
            * score_scale
        )
        grad_values = jnp.einsum(
            "hqk,qhd->khd",
            attn_weights.astype(jnp.bfloat16),
            grad_heads,
            preferred_element_type=jnp.float32,
        )
        return jnp.concatenate(
            [
                grad_keys.reshape(block_len, model_width),
                grad_values.reshape(block_len, model_width),
            ],
            1,
        )

    def query_term(grad_scores, key_block):
        return (
            jnp.einsum("hqk,khd->qhd", grad_scores, key_block, preferred_element_type=jnp.float32)
            * score_scale
        )

    group_rows = group_graphs.shape[0]

    def add_piece(carried, kv_piece, first_row):
        key_piece, value_piece = kv_piece
        piece_rows = key_piece.shape[0]
        block_len = block_length(piece_rows, BLOCK_CAP)

        def add_block(block_state, block_index):
            grad_query, buffer = block_state
            block_start = block_index * block_len
            key_block = lax.dynamic_slice_in_dim(key_piece, block_start, block_len, 0).reshape(
                block_len, HEADS, HEAD_DIM
            )
            value_block = lax.dynamic_slice_in_dim(value_piece, block_start, block_len, 0).reshape(
                block_len, HEADS, HEAD_DIM
            )
            place = first_row + block_start
            key_graphs = lax.dynamic_slice_in_dim(group_graphs, place, block_len, 0)
            attn_weights, grad_scores = score_block(key_block, value_block, key_graphs)
            grad_query = grad_query + query_term(grad_scores, key_block)
            block_terms = key_terms(attn_weights, grad_scores, block_len)
            current = lax.dynamic_slice_in_dim(buffer, place, block_len, 0)
            buffer = lax.dynamic_update_slice_in_dim(buffer, current + block_terms, place, 0)
            return ((grad_query, buffer), None)

        carried, _ = lax.scan(add_block, carried, jnp.arange(piece_rows // block_len))
        return carried

    start_state = (
        jnp.zeros((row_count, HEADS, HEAD_DIM), jnp.float32),
        jnp.zeros((group_rows, 2 * model_width), jnp.float32),
    )
    grad_query, buffer = add_piece(
        start_state,
        (
            lax.all_gather(key_rows, "nodes", axis=0, tiled=True),
            lax.all_gather(value_rows, "nodes", axis=0, tiled=True),
        ),
        jnp.int32(0),
    )
    grad_kv = lax.psum_scatter(buffer, "nodes", scatter_dimension=0, tiled=True)
    return (
        grad_query.reshape(row_count, model_width),
        grad_kv[:, :model_width],
        grad_kv[:, model_width:],
    )


def layer_forward(
    hidden, params, edge_feat, edge_src, edge_dst, halo_send, local_graphs, group_graphs, node_total
):
    w_proj, w_edge, w_qkv, w_out, w_up, w_down, norm_gains, norm_shifts = params
    row_count, model_width = hidden.shape
    hidden_low = hidden.astype(jnp.bfloat16)
    projected = forward_product(hidden_low, w_proj)
    self_term = projected[:, :model_width]
    dest_term = projected[:, 2 * model_width : 3 * model_width]
    source_rows = jnp.concatenate(
        [projected[:, model_width : 2 * model_width], projected[:, 3 * model_width :]], 1
    ).astype(jnp.bfloat16)
    incoming = exchange_sources(source_rows[halo_send])
    extended = jnp.concatenate([source_rows, incoming], 0)
    edge_rows = extended[edge_src].astype(jnp.float32)
    source_b = edge_rows[:, :model_width]
    source_e = edge_rows[:, model_width:]
    edge_proj = forward_product(edge_feat, w_edge)
    gating = jax.nn.sigmoid(dest_term[edge_dst] + source_e + edge_proj)
    numerator = jax.ops.segment_sum(gating * source_b, edge_dst, row_count)
    denominator = jax.ops.segment_sum(gating, edge_dst, row_count)
    message = self_term + numerator / (denominator + GATE_EPS)
    normed_one, standard_one, inv_one = normalize(
        message, norm_gains[0], norm_shifts[0], node_total
    )
    local_out = hidden + jax.nn.silu(normed_one)
    qkv_low = forward_product(hidden_low, w_qkv).astype(jnp.bfloat16)
    query_rows = qkv_low[:, :model_width]
    key_rows = qkv_low[:, model_width : 2 * model_width]
    value_rows = qkv_low[:, 2 * model_width :]
    attn_raw, log_sum = attend_forward(query_rows, key_rows, value_rows, local_graphs, group_graphs)
    attn_low = attn_raw.reshape(row_count, model_width).astype(jnp.bfloat16)
    attn_proj = forward_product(attn_low, w_out)
    normed_two, standard_two, inv_two = normalize(
        hidden + attn_proj, norm_gains[1], norm_shifts[1], node_total
    )
    mixed = local_out + normed_two
    mixed_low = mixed.astype(jnp.bfloat16)
    up_proj = forward_product(mixed_low, w_up)
    activated = jax.nn.silu(up_proj).astype(jnp.bfloat16)
    down_proj = forward_product(activated, w_down)
    normed_three, standard_three, inv_three = normalize(
        mixed + down_proj, norm_gains[2], norm_shifts[2], node_total
    )
    saved = (
        hidden_low,
        source_b,
        gating,
        numerator,
        denominator,
        normed_one,
        standard_one,
        inv_one,
        query_rows,
        key_rows,
        value_rows,
        attn_raw,
        log_sum,
        attn_low,
        standard_two,
        inv_two,
        mixed_low,
        up_proj,
        activated,
        standard_three,
        inv_three,
    )
    return (normed_three, saved)


def layer_backward(
    grad_out,
    params,
    saved,
    edge_feat,
    edge_src,
    edge_dst,
    halo_send,
    local_graphs,
    group_graphs,
    node_total,
):
    w_proj, w_edge, w_qkv, w_out, w_up, w_down, norm_gains, norm_shifts = params
    (
        hidden_low,
        source_b,
        gating,
        numerator,
        denominator,
        normed_one,
        standard_one,
        inv_one,
        query_rows,
        key_rows,
        value_rows,
        attn_raw,
        log_sum,
        attn_low,
        standard_two,
        inv_two,
        mixed_low,
        up_proj,
        activated,
        standard_three,
        inv_three,
    ) = saved
    row_count, model_width = grad_out.shape
    grad_three, gain_three, shift_three = normalize_back(
        grad_out, standard_three, inv_three, norm_gains[2], node_total
    )
    down_grad = grad_three.astype(jnp.bfloat16)
    grad_w_down = outer_product(activated, down_grad)
    up_grad = (times_transposed(down_grad, w_down) * silu_slope_plain(up_proj)).astype(jnp.bfloat16)
    grad_w_up = outer_product(mixed_low, up_grad)
    grad_mixed = grad_three + times_transposed(up_grad, w_up)
    grad_two, gain_two, shift_two = normalize_back(
        grad_mixed, standard_two, inv_two, norm_gains[1], node_total
    )
    out_grad = grad_two.astype(jnp.bfloat16)
    grad_w_out = outer_product(attn_low, out_grad)
    attn_grad = times_transposed(out_grad, w_out).astype(jnp.bfloat16)
    grad_query, grad_key, grad_value = attend_backward(
        query_rows, key_rows, value_rows, attn_grad, attn_raw, log_sum, local_graphs, group_graphs
    )
    qkv_grad = jnp.concatenate([grad_query, grad_key, grad_value], 1).astype(jnp.bfloat16)
    grad_w_qkv = outer_product(hidden_low, qkv_grad)
    grad_message, gain_one, shift_one = normalize_back(
        grad_mixed * silu_slope_plain(normed_one), standard_one, inv_one, norm_gains[0], node_total
    )
    shifted = denominator + GATE_EPS
    grad_numer = grad_message / shifted
    grad_denom = -grad_message * numerator / (shifted * shifted)
    numer_edge = grad_numer[edge_dst]
    grad_gate = numer_edge * source_b + grad_denom[edge_dst]
    grad_pre_edge = grad_gate * gating * (1.0 - gating)
    edge_grad = grad_pre_edge.astype(jnp.bfloat16)
    grad_w_edge = outer_product(edge_feat, edge_grad)
    grad_dest = jax.ops.segment_sum(grad_pre_edge, edge_dst, row_count)
    grad_extended = jax.ops.segment_sum(
        jnp.concatenate([numer_edge * gating, grad_pre_edge], 1),
        edge_src,
        row_count + halo_send.shape[0],
    )
    returned = return_sources(grad_extended[row_count:])
    grad_source = grad_extended[:row_count].at[halo_send].add(returned)
    proj_grad = jnp.concatenate(
        [grad_message, grad_source[:, :model_width], grad_dest, grad_source[:, model_width:]], 1
    ).astype(jnp.bfloat16)
    grad_w_proj = outer_product(hidden_low, proj_grad)
    grad_hidden = (
        grad_mixed
        + grad_two
        + times_transposed(proj_grad, w_proj)
        + times_transposed(qkv_grad, w_qkv)
    )
    weight_grads = (grad_w_proj, grad_w_edge, grad_w_qkv, grad_w_out, grad_w_up, grad_w_down)
    return (
        grad_hidden,
        weight_grads,
        jnp.stack([gain_one, gain_two, gain_three]),
        jnp.stack([shift_one, shift_two, shift_three]),
    )


def per_device(
    node_input,
    edge_feat,
    graph_ids,
    edge_src,
    edge_dst,
    halo_send,
    w_proj,
    w_edge,
    w_qkv,
    w_out,
    w_up,
    w_down,
    norm_gain,
    norm_shift,
    cotangent,
):
    group_graphs = lax.all_gather(graph_ids, "nodes", axis=0, tiled=True)
    node_total = node_input.shape[0] * lax.axis_size("nodes") * lax.axis_size("rep")
    layer_count = w_proj.shape[0]
    layer_params = [
        (
            w_proj[layer_index],
            w_edge[layer_index],
            w_qkv[layer_index],
            w_out[layer_index],
            w_up[layer_index],
            w_down[layer_index],
            norm_gain[layer_index],
            norm_shift[layer_index],
        )
        for layer_index in range(layer_count)
    ]
    hidden = node_input.astype(jnp.float32)
    saved_all = []
    for layer_index in range(layer_count):
        hidden, saved = layer_forward(
            hidden,
            layer_params[layer_index],
            edge_feat,
            edge_src,
            edge_dst,
            halo_send,
            graph_ids,
            group_graphs,
            node_total,
        )
        saved_all.append(saved)
    grad_hidden = cotangent.astype(jnp.float32)
    weight_parts = [None] * layer_count
    gain_parts = [None] * layer_count
    shift_parts = [None] * layer_count
    for layer_index in range(layer_count - 1, -1, -1):
        (
            grad_hidden,
            weight_parts[layer_index],
            gain_parts[layer_index],
            shift_parts[layer_index],
        ) = layer_backward(
            grad_hidden,
            layer_params[layer_index],
            saved_all[layer_index],
            edge_feat,
            edge_src,
            edge_dst,
            halo_send,
            graph_ids,
            group_graphs,
            node_total,
        )
    proj_local = jnp.stack([weight_parts[layer_index][0] for layer_index in range(layer_count)])
    edge_local = jnp.stack([weight_parts[layer_index][1] for layer_index in range(layer_count)])
    qkv_local = jnp.stack([weight_parts[layer_index][2] for layer_index in range(layer_count)])
    out_local = jnp.stack([weight_parts[layer_index][3] for layer_index in range(layer_count)])
    up_local = jnp.stack([weight_parts[layer_index][4] for layer_index in range(layer_count)])
    down_local = jnp.stack([weight_parts[layer_index][5] for layer_index in range(layer_count)])
    grad_proj, grad_edge, grad_qkv, grad_out, grad_up, grad_down = lax.psum(
        (proj_local, edge_local, qkv_local, out_local, up_local, down_local), ("nodes", "rep")
    )
    return (
        hidden,
        grad_hidden,
        grad_proj,
        grad_edge,
        grad_qkv,
        grad_out,
        grad_up,
        grad_down,
        jnp.stack(gain_parts),
        jnp.stack(shift_parts),
    )


def solution(mesh):
    in_specs = (
        P(("rep", "nodes"), None),
        P(("rep", "nodes"), None),
        P(("rep", "nodes")),
        P(("rep", "nodes")),
        P(("rep", "nodes")),
        P(("rep", "nodes")),
        P(),
        P(),
        P(),
        P(),
        P(),
        P(),
        P(),
        P(),
        P(("rep", "nodes"), None),
    )
    out_specs = (
        P(("rep", "nodes"), None),
        P(("rep", "nodes"), None),
        P(),
        P(),
        P(),
        P(),
        P(),
        P(),
        P(),
        P(),
    )
    N, M = mesh.shape["nodes"], mesh.shape["rep"]
    fused = N in (4, 8) and M % 2 == 0 and 512 % (16 * N * M) == 0
    return jax.shard_map(
        functools.partial(fused_device, N, M) if fused else per_device,
        mesh=mesh, in_specs=in_specs, out_specs=out_specs, check_vma=False,
    )
```

```python
import functools
import math

import jax
import jax.numpy as jnp
from jax import lax
from jax.experimental import pallas as pl
from jax.experimental.pallas import tpu as pltpu
from jax.sharding import PartitionSpec as P

HEADS = 8
HEAD_DIM = 32
NEG = -1e30
NORM_EPS = 1e-05
GATE_EPS = 1e-06
F32, BF16, I32 = jnp.float32, jnp.bfloat16, jnp.int32
MESH = pl.DeviceIdType.MESH
SYNCS = 12
STRIP = 32
GROUPS = (
    ("early", 1, 0, 2560, ("core", "y", "nodes")),
    ("conv", 1, 0, 2560, ("core", "y", "nodes")),
    ("qkv", 1, 0, 1536, ("core", "y", "nodes")),
    ("early", 0, 0, 2560, ("core", "x", "y", "z")),
    ("conv", 0, 0, 2560, ("core", "y", "nodes")),
    ("qkv", 0, 0, 1024, ("rep", "nodes")),
    ("qkv", 0, 1024, 512, ("nodes", "rep")),
)


def dot(left, right):
    return lax.dot_general(
        left, right, (((1,), (0,)), ((), ())), preferred_element_type=F32
    )


def dot_nt(left, right):
    return lax.dot_general(
        left, right, (((1,), (1,)), ((), ())), preferred_element_type=F32
    )


def dot_tn(left, right):
    return lax.dot_general(
        left, right, (((0,), (0,)), ((), ())), preferred_element_type=F32
    )


def split(value):
    high = value.astype(BF16)
    return high, (value - high.astype(F32)).astype(BF16)


def sigmoid(value):
    return jax.nn.sigmoid(value)


def silu_slope(value):
    logistic = sigmoid(value)
    return logistic * (1.0 + value * (1.0 - logistic))


def col_sum(value):
    return jnp.sum(value, axis=0, keepdims=True)


def pack(first, second):
    return jnp.concatenate([first[:, :128], first[:, 128:], second[:, :128], second[:, 128:]], 0)


def unpack(tile):
    return [jnp.concatenate([tile[i : i + 1], tile[i + 1 : i + 2]], 1) for i in (0, 2)]


def combine_moments(tiles, count):
    mean = jnp.mean(tiles[:, 0:2], 0)
    off = tiles[:, 0:2] - mean
    return jnp.concatenate([mean, jnp.sum(tiles[:, 2:4] + count * off * off, 0)], 0)


class Refs:
    pass


def axis_sizes(N, M):
    return dict(core=2, y=M // 2, x=2, z=N // 2, rep=M, nodes=N)


def scratch_list(N, M, L, R, E):
    NZ, NB, G = N // 2, N // 4, N * R
    D, FF, W, HH = 256, 512, 4 * R, HEADS // 2 * R
    dma = lambda *shape: pltpu.SemaphoreType.DMA(shape)
    vm = lambda dtype, *shape: pltpu.VMEM(shape, dtype)
    names = dict(
        gb=vm(BF16, L, N, R, D),
        xs=vm(BF16, L, N, R, D),
        meta=vm(I32, N, 8, 256),
        cot=vm(BF16, R, D),
        wp=vm(BF16, L, D, 4 * D),
        we=vm(BF16, L, D, D),
        wqkv=vm(BF16, L, D, 3 * D),
        wo=vm(BF16, L, D, D),
        wu=vm(BF16, L, D, FF),
        wd=vm(BF16, L, FF, D),
        st1=vm(F32, SYNCS, M * N, 4, 128),
        gain=vm(F32, L, 8, D),
        shift=vm(F32, L, 8, D),
        ggain=vm(F32, L, 8, D),
        gshift=vm(F32, L, 8, D),
        iv=vm(F32, L, 8, D),
        moff=vm(F32, N, 8, D),
        move=vm(F32, 8, D),
        le=vm(BF16, E, 1024),
        re=vm(BF16, 1024, D),
        TT=vm(BF16, R, 2 * E),
        ST=vm(BF16, 256, E),
        efT=vm(BF16, D, E),
        HP=vm(BF16, 32, R),
        HN=vm(BF16, 32, R),
        A=vm(BF16, R, 64),
        bias=vm(F32, R, G),
        xf=vm(F32, L + 1, R, D),
        xe=vm(BF16, L, 256, D),
        xeT=vm(BF16, D, 256),
        gate=vm(F32, L, E, D),
        bs=vm(BF16, L, E, D),
        num=vm(F32, L, R, D),
        den=vm(F32, L, R, D),
        z0=vm(F32, L, R, D),
        z1=vm(F32, L, R, D),
        z2=vm(F32, L, R, D),
        wkvT=vm(BF16, L, 2 * D, D),
        kvT=vm(BF16, L, 2 * D, G),
        odT=vm(F32, NB, D, R),
        ldT=vm(F32, NB, D, R),
        md=vm(F32, NB, R, D),
        rb=vm(F32, L, NB, R, D),
        pst=vm(BF16, L, HEADS * R, G),
        oraw=vm(F32, L, R, D),
        ob=vm(BF16, L, R, D),
        mb=vm(BF16, L, R, D),
        u=vm(F32, L, R, FF),
        g=vm(BF16, L, R, FF),
        dy=vm(F32, R, D),
        dmix=vm(F32, R, D),
        gy0=vm(F32, R, D),
        local=vm(F32, R, D),
        dxo=vm(F32, R, D),
        dob=vm(F32, R, D),
        dqT=vm(F32, D, R),
        qm=vm(BF16, L, 2, HH, 128),
        q=vm(BF16, L, R, D),
        qT=vm(BF16, D, R),
        dosT=vm(BF16, 128, R),
        dom=vm(BF16, HH, 256),
        sc=vm(F32, 2, max(2 * R, E), W),
        tp=vm(F32, HEADS // 2, R, 128),
        dss=vm(BF16, HH, W),
        dkv=vm(BF16, 2 * D, W),
        gkv=vm(F32, 2 * D, D),
        gg=vm(BF16, 2 * E, 2 * D),
        dn=vm(BF16, 512, 2 * D),
        dproj=vm(BF16, 256, 4 * D),
        dxs=vm(BF16, L, NZ, 2, R, D),
        rs1=vm(BF16, L, NZ, R, D),
        cs=vm(BF16, L, NZ, R, D),
        rs2=vm(BF16, L, NZ, R, D),
        ro=vm(BF16, L, 3, R, D),
        hs=vm(BF16, L, 2, 32, D),
        hr=vm(BF16, L, 2, 32, D),
    )
    names.update(
        gs_early=vm(BF16, L, 2560, 128),
        gs_conv=vm(BF16, L, 2560, 128),
        gs_qkv=vm(BF16, L, 1536, 128),
    )
    sizes = axis_sizes(N, M)
    for g, (_, _, _, rows, stages) in enumerate(GROUPS):
        names[f"go{g}"] = vm(BF16, rows, 128)
        left = rows
        for k, axis in enumerate(stages):
            left //= sizes[axis]
            names[f"ga{g}_{k}"] = vm(BF16, sizes[axis] - 1, left, 128)
            if k < len(stages) - 1:
                names[f"gh{g}_{k}"] = vm(BF16, left, 128)
    names.update(
        ar_s=dma(len(GROUPS)),
        ar_r=dma(sum(2 * len(stages) for *_, stages in GROUPS)),
        ar_l=dma(len(GROUPS)),
        load=dma(9),
        store=dma(2),
        meta_s=dma(1),
        meta_r=dma(1),
        st_s=dma(1),
        st_r=dma(SYNCS),
        ag_s=dma(1),
        agn_r=dma(L),
        agc_r=dma(L, NZ),
        agp_r=dma(L),
        rs_s=dma(1),
        rsp_r=dma(L, NB, 2),
        ro_r=dma(L),
        rsc_r=dma(L),
        hal_s=dma(1),
        hal_r=dma(L),
    )
    return names


IN_NAMES = (
    "x_in", "ids", "edge_src", "edge_dst", "halo", "ef_h", "wp_h", "we_h", "wqkv_h", "wo_h", "wu_h", "wd_h",
    "gain_in", "shift_in", "cot_h",
)
OUT_NAMES = ("out_act", "grad_in", *(f"gout{g}" for g in range(len(GROUPS))), "ggain_out", "gshift_out")


def kernel(N, M, L, names, *args):
    r_ = Refs()
    for name, ref in zip(IN_NAMES + OUT_NAMES + tuple(names), args, strict=True):
        setattr(r_, name, ref)
    R, D = r_.x_in.shape
    E = r_.ef_h.shape[0]
    NZ, NB, G, W = N // 2, N // 4, N * R, 4 * R
    HK = HEADS // 2
    total = float(N * M * R)
    scale = HEAD_DIM ** -0.5
    me = lax.axis_index("nodes")
    rep = lax.axis_index("rep")
    z = me // 2
    par = me % 2
    partner = 2 * z + (1 - par)
    prev = (me + N - 1) % N
    nxt = (me + 1) % N
    zh, zl = z // 2, z % 2
    z_to = lambda t: 2 * ((zh + t // 2) % NB) + (zl + t % 2) % 2
    z_from = lambda t: 2 * ((zh + NB - t // 2) % NB) + (zl + t % 2) % 2

    def remote(src, dst, s_sem, r_sem, **where):
        return pltpu.make_async_remote_copy(
            src_ref=src, dst_ref=dst, send_sem=s_sem, recv_sem=r_sem,
            device_id=where, device_id_type=MESH,
        )

    def send(src, dst, s_sem, r_sem, **where):
        remote(src, dst, s_sem, r_sem, **where).start()

    def send_rows(src, dst, rows, s_sem, r_sem, **where):
        pieces = next(p for p in range(1, rows) if rows % (16 * p) == 0 and rows // p <= 128)
        for at in range(0, rows, rows // pieces):
            cut = pl.ds(at, rows // pieces)
            send(src.at[cut], dst.at[cut], s_sem, r_sem, **where)

    def arrive(dst, r_sem):
        remote(dst, dst, r_sem, r_sem, nodes=partner).wait_recv()

    def sent(src, s_sem):
        remote(src, src, s_sem, s_sem, nodes=partner).wait_send()

    def when(condition, *acts):
        if condition:
            for act in acts:
                act()

    loads = [pltpu.make_async_copy(r_.ef_h, r_.le.at[:, D : 2 * D], r_.load.at[0])] + [
        pltpu.make_async_copy(getattr(r_, f"{name}_h"), getattr(r_, name), r_.load.at[1 + i])
        for i, name in enumerate(("we", "wqkv", "wp", "wo", "wu", "wd", "cot"))
    ]
    own_rows = pltpu.make_async_copy(r_.x_in, r_.gb.at[0, me], r_.load.at[8])
    own_rows.start()
    for load in loads:
        load.start()

    barrier = pltpu.get_barrier_semaphore()
    for dr in range(M):
        for d in range(N):
            if dr + d > 0:
                pl.semaphore_signal(barrier, inc=1, device_id={"rep": (rep + dr) % M, "nodes": (me + d) % N},
                                    device_id_type=MESH)
    pl.semaphore_wait(barrier, M * N - 1)

    def gather_start(l):
        mine = r_.gb.at[l, me]
        for t in range(2, NZ):
            send_rows(mine, mine, R, r_.ag_s.at[0], r_.agc_r.at[l, t], nodes=2 * z_to(t) + par)
        send_rows(mine, mine, R, r_.ag_s.at[0], r_.agn_r.at[l], nodes=partner)
        send_rows(mine, mine, R, r_.ag_s.at[0], r_.agn_r.at[l], nodes=2 * z_to(1) + par)
        send_rows(mine, mine, R, r_.ag_s.at[0], r_.agn_r.at[l], nodes=2 * z_to(1) + 1 - par)

    def gather_pass(l, t):
        piece = r_.gb.at[l, 2 * z_from(t) + par]
        arrive(piece, r_.agc_r.at[l, t])
        send_rows(piece, piece, R, r_.ag_s.at[0], r_.agp_r.at[l], nodes=partner)

    def gather_near(l):
        arrive(r_.gb.at[l, 0:3], r_.agn_r.at[l])

    def gather_far(l):
        arrive(r_.gb.at[l, 0 : NZ - 2], r_.agp_r.at[l])

    def sync_start(k, first, second):
        mine = rep * N + me
        r_.st1[k, mine] = pack(first, second)
        for dr in range(M):
            for d in range(N):
                if dr + d > 0:
                    send(r_.st1.at[k, mine], r_.st1.at[k, mine], r_.st_s.at[0], r_.st_r.at[k],
                         rep=(rep + dr) % M, nodes=(me + d) % N)

    def sync_wait(k):
        arrive(r_.st1.at[k, 0 : M * N - 1], r_.st_r.at[k])

    def sync_moments(k):
        sync_wait(k)
        return unpack(combine_moments(r_.st1[k], float(R)))

    def sync_sums(k):
        sync_wait(k)
        return unpack(jnp.sum(r_.st1[k], 0))

    sizes = axis_sizes(N, M)
    core, row = rep % 2, rep // 2
    places = dict(
        core=(core, lambda t: dict(rep=2 * row + t)),
        y=(row, lambda t: dict(rep=2 * t + core)),
        x=(par, lambda t: dict(nodes=2 * z + t)),
        z=(z, lambda t: dict(nodes=2 * t + par)),
        rep=(rep, lambda t: dict(rep=t)),
        nodes=(me, lambda t: dict(nodes=t)),
    )

    def reduce_step(g, step):
        name, layer, first, rows, stages = GROUPS[g]
        K = len(stages)
        base = sum(2 * len(before) for *_, before in GROUPS[:g])
        gs, out = getattr(r_, f"gs_{name}").at[layer, first : first + rows], getattr(r_, f"go{g}")
        count, offset = [rows], [0]
        for axis in stages:
            count.append(count[-1] // sizes[axis])
            offset.append(offset[-1] + places[axis][0] * count[-1])
        take = lambda start, size: pl.ds(pl.multiple_of(start, 16), size)
        if 1 <= step <= K:
            k = step - 1
            got = getattr(r_, f"ga{g}_{k}")
            arrive(got, r_.ar_r.at[base + k])
            held = gs if k == 0 else getattr(r_, f"gh{g}_{k - 1}")
            index = places[stages[k]][0]
            acc = held[take(index * count[k + 1], count[k + 1])].astype(F32)
            for slot in range(sizes[stages[k]] - 1):
                acc = acc + got[slot].astype(F32)
            if step < K:
                getattr(r_, f"gh{g}_{k}")[...] = acc.astype(BF16)
            else:
                out[take(offset[K], count[K])] = acc.astype(BF16)
        elif step > K:
            k = 2 * K - step
            arrive(out.at[0 : (sizes[stages[k]] - 1) * count[k + 1]], r_.ar_r.at[base + step - 1])
        if step < K:
            held = gs if step == 0 else getattr(r_, f"gh{g}_{step - 1}")
            index, device = places[stages[step]]
            size = sizes[stages[step]]
            for d in range(1, size):
                to = (index + d) % size
                send_rows(held.at[take(to * count[step + 1], count[step + 1])], getattr(r_, f"ga{g}_{step}").at[d - 1],
                     count[step + 1], r_.ar_s.at[g], r_.ar_r.at[base + step], **device(to))
        elif step < 2 * K:
            k = 2 * K - 1 - step
            index, device = places[stages[k]]
            size = sizes[stages[k]]
            here = out.at[take(offset[k + 1], count[k + 1])]
            for d in range(1, size):
                send_rows(here, here, count[k + 1], r_.ar_s.at[g], r_.ar_r.at[base + step],
                          **device((index + d) % size))
        else:
            pltpu.make_async_copy(out, getattr(r_, f"gout{g}"), r_.ar_l.at[g]).start()

    def reduce_drain(g):
        name, _, _, rows, _ = GROUPS[g]
        sent(getattr(r_, f"gs_{name}").at[:, 0 : rows - rows // (M * N)], r_.ar_s.at[g])
        pltpu.make_async_copy(getattr(r_, f"go{g}"), getattr(r_, f"gout{g}"), r_.ar_l.at[g]).wait()

    def put(buf, l, at, value):
        rows = value.shape[0]
        for c in range(value.shape[1] // 128):
            buf[l, at : at + rows] = value[:, 128 * c : 128 * (c + 1)].astype(BF16)
            at += rows
        return at

    lane_head = lax.broadcasted_iota(I32, (R, 128), 1) // HEAD_DIM

    def by_head(parts):
        out = parts[0]
        for k in range(1, HK):
            out = jnp.where(lane_head == k, parts[k], out)
        return out

    r_.meta[me] = jnp.full((8, 256), -1, I32)
    r_.meta[me, 0:1, 0:R] = r_.ids[...].reshape(1, R)
    r_.meta[me, 1:2, 0:48] = r_.halo[...].reshape(1, 48)
    for d in range(1, N):
        send(r_.meta.at[me], r_.meta.at[me], r_.meta_s.at[0], r_.meta_r.at[0], nodes=(me + d) % N)
    own_rows.wait()
    gather_start(0)

    src_row = r_.edge_src[...].reshape(1, E)
    src_row = jnp.where(src_row < R + 24, src_row, src_row + 8)
    dst_row = r_.edge_dst[...].reshape(1, E)
    src_col = jnp.broadcast_to(src_row, (128, E)).T[:, 0:1]
    dst_col = jnp.broadcast_to(dst_row, (128, E)).T[:, 0:1]
    as_mask = lambda cond: cond.astype(F32).astype(BF16)
    r_.le[:, 0:256] = as_mask(src_col == lax.broadcasted_iota(I32, (E, 256), 1))
    target = as_mask(dst_col == lax.broadcasted_iota(I32, (E, 256), 1))
    r_.le[:, 512:768] = target
    r_.le[:, 768:1024] = target
    target = as_mask(dst_row == lax.broadcasted_iota(I32, (R, E), 0))
    r_.TT[:, 0:E] = target
    r_.TT[:, E:] = target
    r_.ST[...] = as_mask(src_row == lax.broadcasted_iota(I32, (256, E), 0))
    r_.dn[R:256] = jnp.zeros((256 - R, 2 * D), BF16)
    r_.dn[256 + R : 512] = jnp.zeros((256 - R, 2 * D), BF16)
    r_.dproj[R:256, 0:D] = jnp.zeros((256 - R, D), BF16)
    r_.dproj[R:256, 2 * D : 3 * D] = jnp.zeros((256 - R, D), BF16)
    loads[0].wait()
    r_.efT[...] = r_.le[:, D : 2 * D].T
    for l in range(L):
        for k in range(3):
            r_.gain[l, k : k + 1] = r_.gain_in[k, l : l + 1]
            r_.shift[l, k : k + 1] = r_.shift_in[k, l : l + 1]
    r_.xf[0] = r_.gb[0, me].astype(F32)
    r_.moff[...] = jnp.zeros((N, 8, D), F32)
    r_.move[0:1] = jnp.ones((1, D), F32)
    r_.move[1:2] = jnp.zeros((1, D), F32)
    for load in loads[1:]:
        load.wait()
    for l in range(L):
        r_.wkvT[l] = r_.wqkv[l, :, D:].T

    arrive(r_.meta.at[0 : N - 1], r_.meta_r.at[0])
    id_col = jnp.broadcast_to(r_.meta[me][0:1, 0:R], (128, R)).T[:, 0:1]
    id_row = jnp.concatenate(
        [r_.meta[4 * ((zh + NB - j // 4) % NB) + j % 4][0:1, 0:R] for j in range(N)], 1
    )
    r_.bias[...] = jnp.where(id_col == id_row, 0.0, NEG)

    def halo_onehot(device, start):
        col = jnp.broadcast_to(r_.meta[device][1:2, 0:128], (128, 128)).T[start : start + 24, 0:1]
        hot = (col == lax.broadcasted_iota(I32, (24, R), 1)).astype(F32)
        return jnp.concatenate([hot, jnp.zeros((8, R), F32)], 0).astype(BF16)

    r_.HP[...] = halo_onehot(prev, 24)
    r_.HN[...] = halo_onehot(nxt, 0)
    r_.A[...] = as_mask(r_.meta[me][1:2, 0:64] == lax.broadcasted_iota(I32, (R, 64), 0))

    factor_exp = scale * math.log2(math.e)

    def prepare_queries(l):
        q = dot(r_.xs[l, me], r_.wqkv[l, :, :D]).astype(BF16)
        r_.q[l] = q
        q = q.astype(F32)
        for hf in range(2):
            for k in range(HK):
                part = jnp.where(lane_head == k, q[:, 128 * hf : 128 * (hf + 1)], 0.0)
                r_.qm[l, hf, k * R : (k + 1) * R] = part.astype(BF16)

    def head_dims(hf, k, base=0):
        first = base + hf * 128 + k * HEAD_DIM
        return slice(first, first + HEAD_DIM)

    def head_rows(hf, k, count=1):
        return slice((hf * HK + k) * R, (hf * HK + k + count) * R)

    def lane_half(hf):
        return slice(hf * 128, (hf + 1) * 128)

    def half_of(i):
        return (zh + NB - i) % NB, slice(i * W, (i + 1) * W)

    def attention_keys(l, i):
        half, rows = half_of(i)
        x = r_.xs[l, pl.ds(4 * half, 4)].reshape(W, D)
        r_.kvT[l, :, rows] = dot_nt(r_.wkvT[l], x).astype(BF16)

    def attention_heads(l, i, hfs):
        _, rows = half_of(i)
        for hf in hfs:
            lanes = lane_half(hf)
            ones = jnp.ones((HEAD_DIM, W), BF16)
            for c in range(HK // 2):
                r_.sc[c % 2, 0 : 2 * R] = dot(r_.qm[l, hf, 2 * c * R : 2 * (c + 1) * R], r_.kvT[l, lanes, rows])
                for k in range(2):
                    for at in range(0, R, STRIP):
                        s = r_.sc[c % 2, k * R + at : k * R + at + STRIP] + r_.bias[at : at + STRIP, rows]
                        top = jnp.max(s, 1, keepdims=True)
                        e = jnp.exp2((s - top) * factor_exp)
                        r_.tp[2 * c + k, at : at + STRIP] = jnp.broadcast_to(top, (STRIP, 128))
                        first = (hf * HK + 2 * c + k) * R + at
                        r_.pst[l, first : first + STRIP, rows] = e.astype(BF16)
                for k in range(2):
                    h = 2 * c + k
                    left = jnp.concatenate([r_.kvT[l, head_dims(hf, h, D), rows], ones], 0)
                    o = dot_nt(left, r_.pst[l, head_rows(hf, h), rows])
                    r_.odT[i, head_dims(hf, h)] = o[0:HEAD_DIM]
                    r_.ldT[i, head_dims(hf, h)] = o[HEAD_DIM:]
            r_.md[i, :, lanes] = by_head([r_.tp[k] for k in range(HK)])

    def attention_end(l):
        tops = [r_.md[i].T for i in range(NB)]
        top = tops[0]
        for i in range(1, NB):
            top = jnp.maximum(top, tops[i])
        factors = [jnp.exp2((tops[i] - top) * factor_exp) for i in range(NB)]
        inv = 1.0 / sum(factors[i] * r_.ldT[i] for i in range(NB))
        o = jnp.zeros((D, R), F32)
        for i in range(NB):
            r_.rb[l, i] = (factors[i] * inv).T
            o = o + factors[i] * inv * r_.odT[i]
        o = o.T
        r_.oraw[l] = o
        ob = o.astype(BF16)
        r_.ob[l] = ob
        t1 = r_.xf[l] + dot(ob, r_.wo[l])
        r_.z1[l] = t1
        mean1 = col_sum(t1) / R
        return mean1, col_sum((t1 - mean1) * (t1 - mean1))

    def convolution(l):
        xs = r_.xs
        xb = xs[l, me]
        r_.xe[l, 0:R] = xb
        r_.xe[l, R : R + 32] = dot(r_.HP[...], xs[l, prev]).astype(BF16)
        r_.xe[l, R + 32 : R + 64] = dot(r_.HN[...], xs[l, nxt]).astype(BF16)
        xe = r_.xe[l]
        made = dot(xe, r_.wp[l])
        pd_high, pd_low = split(made[:, 2 * D : 3 * D])
        r_.re[0:256] = made[:, 3 * D :].astype(BF16)
        r_.re[256:512] = r_.we[l]
        r_.re[512:768] = pd_high
        r_.re[768:1024] = pd_low
        r_.gate[l] = dot(r_.le[...], r_.re[...])
        r_.bs[l] = dot(r_.le[:, 0:256], made[:, D : 2 * D].astype(BF16)).astype(BF16)
        for at in range(0, E, 64):
            here = slice(at, at + 64)
            gate = sigmoid(r_.gate[l, here])
            r_.gate[l, here] = gate
            high, low = split(jnp.concatenate([gate * r_.bs[l, here].astype(F32), gate], 1))
            r_.gg[here] = high
            r_.gg[E + at : E + at + 64] = low
        num_den = dot(r_.TT[...], r_.gg[...])
        pa, num, den = made[0:R, 0:D], num_den[:, 0:D], num_den[:, D:]
        r_.num[l] = num
        r_.den[l] = den
        msg = pa + num / (den + GATE_EPS)
        r_.z0[l] = msg
        mean0 = col_sum(msg) / R
        return mean0, col_sum((msg - mean0) * (msg - mean0))

    def forward(l):
        def ready(js):
            for j in js:
                moved = (r_.gb[l, j].astype(F32) + r_.moff[j, 0:1]) * r_.move[0:1] + r_.move[1:2]
                r_.xs[l, j] = moved.astype(BF16)

        r_.xs[l, me] = r_.xf[l].astype(BF16)
        prepare_queries(l)
        for t in range(2, NZ):
            gather_pass(l, t)
        gather_near(l)
        ready([partner, 2 * z_from(1) + par, 2 * z_from(1) + 1 - par])

        attention_keys(l, 0)
        attention_heads(l, 0, (0, 1))
        gather_far(l)
        ready([2 * z_from(t) + p for t in range(2, NZ) for p in range(2)])
        mean0, sq0 = convolution(l)
        for i in range(1, NB):
            attention_keys(l, i)
            attention_heads(l, i, (0, 1))
        sync_start(3 * l, mean0, sq0)
        mean1, sq1 = attention_end(l)
        sync_start(3 * l + 1, mean1, sq1)
        mean0, sq0 = sync_moments(3 * l)
        inv0 = lax.rsqrt(sq0 / total + NORM_EPS)
        r_.iv[l, 0:1] = inv0
        z0 = (r_.z0[l] - mean0) * inv0
        r_.z0[l] = z0
        n0 = z0 * r_.gain[l, 0:1] + r_.shift[l, 0:1]
        r_.local[...] = r_.xf[l] + n0 * sigmoid(n0)
        mean1, sq1 = sync_moments(3 * l + 1)
        inv1 = lax.rsqrt(sq1 / total + NORM_EPS)
        r_.iv[l, 1:2] = inv1
        z1 = (r_.z1[l] - mean1) * inv1
        r_.z1[l] = z1
        mix = r_.local[...] + z1 * r_.gain[l, 1:2] + r_.shift[l, 1:2]
        mb = mix.astype(BF16)
        r_.mb[l] = mb
        u = dot(mb, r_.wu[l])
        r_.u[l] = u
        g = (u * sigmoid(u)).astype(BF16)
        r_.g[l] = g
        y = mix + dot(g, r_.wd[l])
        r_.z2[l] = y
        mean = col_sum(y) / R
        cent = y - mean
        k = 3 * l + 2
        sync_start(k, mean, col_sum(cent * cent))

        if l < L - 1:
            r_.gb[l + 1, me] = cent.astype(BF16)
            gather_start(l + 1)

        if l == L - 1:
            dy = r_.cot[...].astype(F32)
            sync_start(3 * L, col_sum(dy), col_sum(dy * cent))

        tot_mean, tot_sq = sync_moments(k)
        inv2 = lax.rsqrt(tot_sq / total + NORM_EPS)
        r_.iv[l, 2:3] = inv2
        z2 = (r_.z2[l] - tot_mean) * inv2
        r_.z2[l] = z2
        gain, shift = r_.gain[l, 2:3], r_.shift[l, 2:3]
        r_.xf[l + 1] = z2 * gain + shift

        if l == L - 1:
            sync_wait(3 * L)
            sums, means = r_.st1[3 * L], r_.st1[k][:, 0:2]
            mean = jnp.mean(means, 0)
            dy_sum = jnp.sum(sums[:, 0:2], 0)
            dy_cent = jnp.sum(sums[:, 2:4] + (means - mean) * sums[:, 0:2], 0)
            dy_sum, dy_cent = unpack(jnp.concatenate([dy_sum, dy_cent], 0))
            r_.gshift[l, 2:3] = dy_sum
            r_.ggain[l, 2:3] = dy_cent * inv2

        for j in range(N):
            tile = r_.st1[k, rep * N + j]
            r_.moff[j, 0:1] = jnp.concatenate([tile[0:1], tile[1:2]], 1) - tot_mean
        r_.move[0:1] = inv2 * gain
        r_.move[1:2] = shift

    for l in range(L):
        forward(l)
    act_copy = pltpu.make_async_copy(r_.xf.at[L], r_.out_act, r_.store.at[0])
    act_copy.start()

    def back_feed_forward(l, k):
        s2, g2 = r_.gshift[l, 2:3], r_.ggain[l, 2:3]
        d3 = r_.gain[l, 2:3] * r_.iv[l, 2:3] * (r_.dy[...] - s2 / total - r_.z2[l] * (g2 / total))
        db = d3.astype(BF16)
        dub = (dot_nt(db, r_.wd[l]) * silu_slope(r_.u[l])).astype(BF16)
        dmix = d3 + dot_nt(dub, r_.wu[l])
        r_.dmix[...] = dmix
        n0 = r_.z0[l] * r_.gain[l, 0:1] + r_.shift[l, 0:1]
        gy0 = dmix * silu_slope(n0)
        sync_start(k, col_sum(dmix), col_sum(dmix * r_.z1[l]))
        sync_start(k + 1, col_sum(gy0), col_sum(gy0 * r_.z0[l]))
        r_.gy0[...] = gy0
        at = put(r_.gs_early, l, 512, dot_tn(r_.mb[l], dub))
        put(r_.gs_early, l, at, dot_tn(r_.g[l], db))
        r_.xeT[...] = r_.xe[l].T
        r_.qT[...] = r_.q[l].T

    def back_norms(l, k):
        s1, g1 = sync_sums(k)
        r_.gshift[l, 1:2] = s1
        r_.ggain[l, 1:2] = g1
        dmix = r_.dmix[...]
        d2 = r_.gain[l, 1:2] * r_.iv[l, 1:2] * (dmix - s1 / total - r_.z1[l] * (g1 / total))
        dab = d2.astype(BF16)
        r_.dxo[...] = dmix + d2
        r_.dob[...] = dot_nt(dab, r_.wo[l]).astype(BF16).astype(F32)
        put(r_.gs_early, l, 0, dot_tn(r_.ob[l], dab))
        r_.gkv[...] = jnp.zeros((2 * D, D), F32)
        r_.dqT[...] = jnp.zeros((D, R), F32)

    def back_half(i):
        t1 = (i + 1) % NB
        half = (zh + t1) % NB
        place = (NB - t1) % NB
        return place, half, slice(place * W, (place + 1) * W)

    def back_heads(l, i, hf):
        place, half, rows = back_half(i)
        if True:
            lanes = lane_half(hf)
            dos = r_.dob[:, lanes] * r_.rb[l, place, :, lanes]
            prod = dos * r_.oraw[l, :, lanes]
            for k in range(HK):
                r_.dom[k * R : (k + 1) * R, 0:128] = jnp.where(lane_head == k, dos, 0.0).astype(BF16)
                r_.dom[k * R : (k + 1) * R, 128:256] = jnp.where(lane_head == k, -prod, 0.0).astype(BF16)
            r_.dosT[...] = dos.T.astype(BF16)
            values = slice(D + hf * 128, D + (hf + 1) * 128)
            right = jnp.concatenate([r_.kvT[l, values, rows], jnp.ones((128, W), BF16)], 0)
            for c in range(HK // 2):
                both = slice(2 * c * R, 2 * (c + 1) * R)
                r_.sc[c % 2, 0 : 2 * R] = dot(r_.dom[both], right)
                for k in range(2):
                    for at in range(0, R, STRIP):
                        first = (hf * HK + 2 * c + k) * R + at
                        e = r_.pst[l, first : first + STRIP, rows].astype(F32)
                        ds = e * r_.sc[c % 2, k * R + at : k * R + at + STRIP]
                        r_.dss[(2 * c + k) * R + at : (2 * c + k) * R + at + STRIP] = ds.astype(BF16)
                for k in range(2):
                    h = 2 * c + k
                    mine, dims = slice(h * R, (h + 1) * R), head_dims(hf, h)
                    r_.dqT[dims] += dot_nt(r_.kvT[l, dims, rows], r_.dss[mine])
                    r_.dkv[dims] = (dot(r_.qT[dims], r_.dss[mine]) * scale).astype(BF16)
                    dv = dot(r_.dosT[h * HEAD_DIM : (h + 1) * HEAD_DIM], r_.pst[l, head_rows(hf, h), rows])
                    r_.dkv[head_dims(hf, h, D)] = dv.astype(BF16)

    def back_rows(l, i):
        _, half, _ = back_half(i)
        dx = dot(r_.wqkv[l, :, D:], r_.dkv[...]).T
        r_.dxs[l, pl.ds(2 * half, 2)] = dx.astype(BF16).reshape(2, 2, R, D)

        if i < NB - 1:
            for low in range(2):
                zb = 2 * half + low
                send_rows(r_.dxs.at[l, zb, 1 - par], r_.rs1.at[l, zb], R,
                     r_.rs_s.at[0], r_.rsp_r.at[l, i, low], nodes=partner)

        else:
            near = z_to(1)
            send_rows(r_.dxs.at[l, z, 1 - par], r_.ro.at[l, 0], R, r_.rs_s.at[0], r_.ro_r.at[l], nodes=partner)
            send_rows(r_.dxs.at[l, near, par], r_.ro.at[l, 1], R, r_.rs_s.at[0], r_.ro_r.at[l], nodes=2 * near + par)
            send_rows(r_.dxs.at[l, near, 1 - par], r_.ro.at[l, 2], R, r_.rs_s.at[0], r_.ro_r.at[l],
                 nodes=2 * near + 1 - par)

        r_.gkv[...] += dot(r_.dkv[...], r_.xs[l, pl.ds(4 * half, 4)].reshape(W, D))

    def pass_on(l, i, t):
        zb = z_to(t)
        arrive(r_.rs1.at[l, zb], r_.rsp_r.at[l, i, zb % 2])
        both = r_.dxs[l, zb, par].astype(F32) + r_.rs1[l, zb].astype(F32)
        r_.cs[l, zb] = both.astype(BF16)
        send_rows(r_.cs.at[l, zb], r_.rs2.at[l, z], R, r_.rs_s.at[0], r_.rsc_r.at[l], nodes=2 * zb + par)

    def back_convolution(l, k):
        s0, g0 = unpack(jnp.sum(r_.st1[k + 1], 0))
        r_.gshift[l, 0:1] = s0
        r_.ggain[l, 0:1] = g0
        inv_den = 1.0 / (r_.den[l] + GATE_EPS)
        dm = r_.gain[l, 0:1] * r_.iv[l, 0:1] * (r_.gy0[...] - s0 / total - r_.z0[l] * (g0 / total))
        dnum = dm * inv_den
        dden = -dnum * r_.num[l] * inv_den
        high, low = split(jnp.concatenate([dnum, dden], 1))
        r_.dn[0:R] = high
        r_.dn[256 : 256 + R] = low
        r_.sc[0, 0:E, 0 : 2 * D] = dot(r_.le[:, 512:1024], r_.dn[...])
        for at in range(0, E, 64):
            here = slice(at, at + 64)
            gate, dnum_e = r_.gate[l, here], r_.sc[0, here, 0:D]
            dgp = (dnum_e * r_.bs[l, here].astype(F32) + r_.sc[0, here, D : 2 * D]) * gate * (1.0 - gate)
            r_.gg[here, 0:D] = (dnum_e * gate).astype(BF16)
            r_.gg[here, D:] = dgp.astype(BF16)
        ext = dot(r_.ST[...], r_.gg[0:E]).astype(BF16)
        r_.dproj[0:R, 0:D] = dm.astype(BF16)
        r_.dproj[:, D : 2 * D] = ext[:, 0:D]
        r_.dproj[0:R, 2 * D : 3 * D] = dot(r_.TT[:, 0:E], r_.gg[0:E, D:]).astype(BF16)
        r_.dproj[:, 3 * D :] = ext[:, D:]
        dxe = dot_nt(r_.dproj[...], r_.wp[l])
        r_.hs[l, 0] = dxe[R : R + 32].astype(BF16)
        r_.hs[l, 1] = dxe[R + 32 : R + 64].astype(BF16)
        r_.dxo[...] += dxe[0:R]

    def send_halo(l):
        send(r_.hs.at[l, 0], r_.hr.at[l, 1], r_.hal_s.at[0], r_.hal_r.at[l], nodes=prev)
        send(r_.hs.at[l, 1], r_.hr.at[l, 0], r_.hal_s.at[0], r_.hal_r.at[l], nodes=nxt)

    def conv_weight_grads(l):
        at = put(r_.gs_conv, l, 0, dot(r_.xeT[...], r_.dproj[...]))
        put(r_.gs_conv, l, at, dot(r_.efT[...], r_.gg[0:E, D:]))

    def back_input(l):
        dx = r_.dxo[...]
        dx = dx + r_.dxs[l, z, par].astype(F32)
        arrive(r_.ro.at[l], r_.ro_r.at[l])
        for slot in range(3):
            dx = dx + r_.ro[l, slot].astype(F32)
        if NZ > 2:
            arrive(r_.rs2.at[l, 0 : NZ - 2], r_.rsc_r.at[l])
        for t in range(2, NZ):
            dx = dx + r_.rs2[l, z_from(t)].astype(F32)
        arrive(r_.hr.at[l], r_.hal_r.at[l])
        back = jnp.concatenate(
            [r_.hr[l, 0].astype(F32)[0:24], r_.hr[l, 1].astype(F32)[0:24], jnp.zeros((16, D), F32)], 0
        )
        return dx + dot(r_.A[...], back.astype(BF16))

    r_.dy[...] = r_.cot[...].astype(F32)

    E1, C1, Q1, E0, C0, QK0, V0 = range(len(GROUPS))

    def steps(*pairs):
        return [functools.partial(reduce_step, g, k) for g, k in pairs]

    r_.dy[...] = r_.cot[...].astype(F32)

    def backward(b):
        l = L - 1 - b
        first, last = b == 0, b == L - 1
        k = 3 * L + 1 + 2 * b
        back_feed_forward(l, k)
        when(last, *steps((E1, 3), (Q1, 2)))
        back_norms(l, k)
        if first:
            when(True, *steps((E1, 0)))
            back_heads(l, 0, 0)
            back_heads(l, 0, 1)
            back_rows(l, 0)
            when(True, *steps((E1, 1)))
            sync_wait(k + 1)
            back_convolution(l, k)
            back_heads(l, 1, 0)
            send_halo(l)
            for t in range(2, NZ):
                pass_on(l, 0, t)
            back_heads(l, 1, 1)
            back_rows(l, 1)
            conv_weight_grads(l)
            when(True, *steps((C1, 0)))
        else:
            when(True, *steps((C1, 3), (E1, 4), (E0, 0)))
            sync_wait(k + 1)
            back_convolution(l, k)
            back_heads(l, 0, 0)
            send_halo(l)
            when(True, *steps((Q1, 3), (E1, 5), (C1, 4), (E0, 1)))
            conv_weight_grads(l)
            back_heads(l, 0, 1)
            back_rows(l, 0)
            when(True, *steps((C0, 0), (E0, 2), (Q1, 4), (E1, 6), (C1, 5)))
            back_heads(l, 1, 0)
            when(True, *steps((C0, 1), (E0, 3), (Q1, 5), (C1, 6)))
            for t in range(2, NZ):
                pass_on(l, 0, t)
            back_heads(l, 1, 1)
            back_rows(l, 1)
            when(True, *steps((C0, 2), (E0, 4), (Q1, 6)))
        dqb = (r_.dqT[...].T * scale).astype(BF16)
        r_.dxo[...] += dot_nt(dqb, r_.wqkv[l, :, 0:D])
        at = put(r_.gs_qkv, l, 0, dot(r_.xeT[:, 0:R], dqb))
        put(r_.gs_qkv, l, at, r_.gkv[...].T)
        if first:
            when(True, *steps((Q1, 0), (C1, 1)))
            dx = back_input(l)
            r_.dy[...] = dx
            below = L - 2
            sync_start(SYNCS - 1, col_sum(dx), col_sum(dx * r_.z2[below]))
            when(True, *steps((E1, 2), (Q1, 1)))
            s2, g2 = sync_sums(SYNCS - 1)
            r_.gshift[below, 2:3] = s2
            r_.ggain[below, 2:3] = g2
            when(True, *steps((C1, 2)))

    for b in range(L):
        backward(b)
    for step in steps((QK0, 0), (V0, 0), (E0, 5), (C0, 3), (V0, 1), (QK0, 1)):
        step()
    r_.dy[...] = back_input(0)
    in_copy = pltpu.make_async_copy(r_.dy, r_.grad_in, r_.store.at[1])
    in_copy.start()
    for step in steps(
        (E0, 6), (C0, 4), (V0, 2), (QK0, 2),
        (E0, 7), (C0, 5), (V0, 3), (QK0, 3),
        (E0, 8), (C0, 6), (V0, 4), (QK0, 4),
    ):
        step()
    for l in range(L):
        for k in range(3):
            r_.ggain_out[k, l : l + 1] = r_.ggain[l, k : k + 1]
            r_.gshift_out[k, l : l + 1] = r_.gshift[l, k : k + 1]
    for g in range(len(GROUPS)):
        reduce_drain(g)
    sent(r_.meta.at[0 : N - 1], r_.meta_s.at[0])
    sent(r_.st1.at[:, 0 : M * N - 1], r_.st_s.at[0])
    sent(r_.gb.at[:, 0 : 3 + 2 * (NZ - 2)], r_.ag_s.at[0])
    sent(r_.gb.at[:, 0 : 2 * (NB - 1) + 3 + NZ - 2], r_.rs_s.at[0])
    sent(r_.hs, r_.hal_s.at[0])
    act_copy.wait()
    in_copy.wait()


def finish_kernel(act_h, gin_h, *refs):
    n = len(GROUPS)
    held, (ggain_h, gshift_h), refs = refs[:n], refs[n : n + 2], refs[n + 2 :]
    act_o, gin_o, proj_o, edge_o, qkv_o, out_o, up_o, down_o, ggain_o, gshift_o = refs[:10]
    summed, refs = refs[10 : 10 + n], refs[10 + n :]
    act, gin, proj, edge, qkv, out, up, down, in_sem, out_sem = refs
    loads = [
        pltpu.make_async_copy(src, dst, in_sem.at[i])
        for i, (src, dst) in enumerate(zip(held + (act_h, gin_h), summed + (act, gin), strict=True))
    ]
    for load in loads:
        load.start()
    ggain_o[...] = ggain_h[...]
    gshift_o[...] = gshift_h[...]
    stores = []

    def store(src, dst):
        copy = pltpu.make_async_copy(src, dst, out_sem.at[len(stores)])
        copy.start()
        stores.append(copy)

    def widen(dst, l, g, at, first=0, last=None):
        rows = dst.shape[1]
        for c in range(first, dst.shape[2] // 128 if last is None else last):
            dst[l, :, 128 * c : 128 * (c + 1)] = summed[g][at : at + rows].astype(F32)
            at += rows
        return at

    for g, (name, l, first, rows, _) in enumerate(GROUPS):
        loads[g].wait()
        if name == "early":
            at = widen(out, l, g, 0)
            store(out.at[l], out_o.at[l])
            at = widen(up, l, g, at)
            store(up.at[l], up_o.at[l])
            widen(down, l, g, at)
            store(down.at[l], down_o.at[l])
        elif name == "conv":
            at = widen(proj, l, g, 0)
            store(proj.at[l], proj_o.at[l])
            widen(edge, l, g, at)
            store(edge.at[l], edge_o.at[l])
        else:
            widen(qkv, l, g, 0, first // 256, (first + rows) // 256)
            if first + rows == 1536:
                store(qkv.at[l], qkv_o.at[l])
    for i, (src, dst) in enumerate(((act, act_o), (gin, gin_o))):
        loads[n + i].wait()
        store(src, dst)
    for copy in stores:
        copy.wait()


def fused_device(
    N, M, node_input, edge_feat, graph_ids, edge_src, edge_dst, halo_send, w_proj, w_edge, w_qkv,
    w_out, w_up, w_down, norm_gain, norm_shift, cotangent,
):
    R, D = node_input.shape
    E = edge_feat.shape[0]
    L = w_proj.shape[0]
    names = scratch_list(N, M, L, R, E)
    vmem = pl.BlockSpec(memory_space=pltpu.VMEM)
    hbm = pl.BlockSpec(memory_space=pltpu.HBM)
    shape = jax.ShapeDtypeStruct
    rows = shape((R, D), F32)
    norm = shape((3, L, D), F32)
    groups = [shape((rows_g, 128), BF16) for _, _, _, rows_g, _ in GROUPS]
    outs = pl.pallas_call(
        functools.partial(kernel, N, M, L, tuple(names)),
        out_shape=[rows, rows, *groups, norm, norm],
        in_specs=[hbm] + [vmem] * 4 + [hbm] * 7 + [vmem] * 2 + [hbm],
        out_specs=[hbm] * (2 + len(GROUPS)) + [vmem] * 2,
        scratch_shapes=list(names.values()),
        compiler_params=pltpu.CompilerParams(
            collective_id=0, has_side_effects=True, vmem_limit_bytes=60 << 20
        ),
        name="layers",
    )(node_input, graph_ids, edge_src, edge_dst, halo_send, edge_feat, w_proj, w_edge, w_qkv, w_out, w_up,
      w_down, norm_gain.transpose(1, 0, 2), norm_shift.transpose(1, 0, 2), cotangent)
    weights = [shape(w.shape, F32) for w in (w_proj, w_edge, w_qkv, w_out, w_up, w_down)]
    results = pl.pallas_call(
        finish_kernel,
        out_shape=[rows, rows, *weights, norm, norm],
        in_specs=[hbm] * (2 + len(GROUPS)) + [vmem] * 2,
        out_specs=[hbm] * 8 + [vmem] * 2,
        scratch_shapes=[pltpu.VMEM(s.shape, s.dtype) for s in (*groups, rows, rows, *weights)]
        + [pltpu.SemaphoreType.DMA((len(GROUPS) + 2,)), pltpu.SemaphoreType.DMA((14,))],
        compiler_params=pltpu.CompilerParams(vmem_limit_bytes=60 << 20),
        name="gradients",
    )(*outs)
    ggain, gshift = results[8].transpose(1, 0, 2), results[9].transpose(1, 0, 2)
    return (*results[:8], ggain, gshift)


BLOCK_CAP = 2048


def extended_2(block, sides, width):
    for axis, dim in sides:
        count = lax.axis_size(axis)
        forward = [(i, i + 1) for i in range(count - 1)]
        forward.append((count - 1, 0))
        backward = [(target, source) for source, target in forward]
        low = lax.ppermute(
            lax.slice_in_dim(block, block.shape[dim] - width, None, axis=dim), axis, forward
        )
        high = lax.ppermute(lax.slice_in_dim(block, 0, width, axis=dim), axis, backward)
        block = jnp.concatenate([low, block, high], axis=dim)
    return block


def block_length(total_rows, upper_limit):
    for length in range(min(total_rows, upper_limit), 0, -1):
        if total_rows % length == 0:
            return length
    return 1


def outer_product(left, right):
    return lax.dot_general(
        left, right, (((0,), (0,)), ((), ())), preferred_element_type=jnp.float32
    )


def times_transposed(left, weight):
    return lax.dot_general(
        left, weight, (((1,), (1,)), ((), ())), preferred_element_type=jnp.float32
    )


def forward_product(left, weight):
    return jnp.dot(left, weight, preferred_element_type=jnp.float32)


def silu_slope_plain(inputs):
    logistic = jax.nn.sigmoid(inputs)
    return logistic * (1.0 + inputs * (1.0 - logistic))


def normalize(inputs, gain_row, shift_row, node_total):
    batch_mean = lax.psum(jnp.sum(inputs, 0), ("nodes", "rep")) / node_total
    centred = inputs - batch_mean
    batch_var = lax.psum(jnp.sum(centred * centred, 0), ("nodes", "rep")) / node_total
    inv_std = lax.rsqrt(batch_var + NORM_EPS)
    standard = (inputs - batch_mean) * inv_std
    return (standard * gain_row + shift_row, standard, inv_std)


def normalize_back(grad_out, standard, inv_std, gain_row, node_total):
    shift_grad, gain_grad = lax.psum(
        (jnp.sum(grad_out, 0), jnp.sum(grad_out * standard, 0)), ("nodes", "rep")
    )
    grad_in = (
        gain_row
        * inv_std
        * (grad_out - shift_grad / node_total - standard * gain_grad / node_total)
    )
    return (grad_in, gain_grad, shift_grad)


def exchange_sources(outgoing):
    halo_rows = outgoing.shape[0] // 2
    grown = extended_2(outgoing, (("nodes", 0),), halo_rows)
    return jnp.concatenate([grown[:halo_rows], grown[3 * halo_rows :]], 0)


def return_sources(incoming_grad):
    halo_rows = incoming_grad.shape[0] // 2
    grown = extended_2(incoming_grad.astype(jnp.bfloat16), (("nodes", 0),), halo_rows).astype(
        incoming_grad.dtype
    )
    return jnp.concatenate([grown[:halo_rows], grown[3 * halo_rows :]], 0)


def attend_forward(query_rows, key_rows, value_rows, local_graphs, group_graphs):
    row_count = query_rows.shape[0]
    score_scale = HEAD_DIM ** (-0.5)
    queries = query_rows.reshape(row_count, HEADS, HEAD_DIM)

    def add_piece(carried, kv_piece, first_row):
        key_piece, value_piece = kv_piece
        piece_rows = key_piece.shape[0]
        block_len = block_length(piece_rows, BLOCK_CAP)

        def add_block(block_state, block_index):
            row_max, row_sum, accumulated = block_state
            block_start = block_index * block_len
            key_block = lax.dynamic_slice_in_dim(key_piece, block_start, block_len, 0).reshape(
                block_len, HEADS, HEAD_DIM
            )
            value_block = lax.dynamic_slice_in_dim(value_piece, block_start, block_len, 0).reshape(
                block_len, HEADS, HEAD_DIM
            )
            key_graphs = lax.dynamic_slice_in_dim(
                group_graphs, first_row + block_start, block_len, 0
            )
            same_graph = (local_graphs[:, None] == key_graphs[None, :])[None]
            scores = (
                jnp.einsum("qhd,khd->hqk", queries, key_block, preferred_element_type=jnp.float32)
                * score_scale
            )
            scores = jnp.where(same_graph, scores, NEG)
            new_max = jnp.maximum(row_max, jnp.max(scores, 2))
            weights = jnp.where(same_graph, jnp.exp(scores - new_max[:, :, None]), 0.0)
            factor = jnp.exp(row_max - new_max)
            row_sum = row_sum * factor + jnp.sum(weights, 2)
            contrib = jnp.einsum(
                "hqk,khd->qhd",
                weights.astype(jnp.bfloat16),
                value_block,
                preferred_element_type=jnp.float32,
            )
            accumulated = accumulated * jnp.transpose(factor)[:, :, None] + contrib
            return ((new_max, row_sum, accumulated), None)

        carried, _ = lax.scan(add_block, carried, jnp.arange(piece_rows // block_len))
        return carried

    start_state = (
        jnp.full((HEADS, row_count), NEG, jnp.float32),
        jnp.zeros((HEADS, row_count), jnp.float32),
        jnp.zeros((row_count, HEADS, HEAD_DIM), jnp.float32),
    )
    row_max, row_sum, accumulated = add_piece(
        start_state,
        (
            lax.all_gather(key_rows, "nodes", axis=0, tiled=True),
            lax.all_gather(value_rows, "nodes", axis=0, tiled=True),
        ),
        jnp.int32(0),
    )
    attn_raw = accumulated / jnp.transpose(row_sum)[:, :, None]
    log_sum = row_max + jnp.log(row_sum)
    return (attn_raw, log_sum)


def attend_backward(
    query_rows, key_rows, value_rows, grad_low, attn_raw, log_sum, local_graphs, group_graphs
):
    row_count = query_rows.shape[0]
    model_width = HEADS * HEAD_DIM
    score_scale = HEAD_DIM ** (-0.5)
    queries = query_rows.reshape(row_count, HEADS, HEAD_DIM)
    grad_heads = grad_low.reshape(row_count, HEADS, HEAD_DIM)
    row_delta = jnp.einsum("qhd,qhd->hq", grad_heads.astype(jnp.float32), attn_raw)

    def score_block(key_block, value_block, key_graphs):
        same_graph = (local_graphs[:, None] == key_graphs[None, :])[None]
        scores = (
            jnp.einsum("qhd,khd->hqk", queries, key_block, preferred_element_type=jnp.float32)
            * score_scale
        )
        attn_weights = jnp.exp(jnp.where(same_graph, scores - log_sum[:, :, None], NEG))
        grad_weights = jnp.einsum(
            "qhd,khd->hqk", grad_heads, value_block, preferred_element_type=jnp.float32
        )
        grad_scores = (attn_weights * (grad_weights - row_delta[:, :, None])).astype(jnp.bfloat16)
        return (attn_weights, grad_scores)

    def key_terms(attn_weights, grad_scores, block_len):
        grad_keys = (
            jnp.einsum("hqk,qhd->khd", grad_scores, queries, preferred_element_type=jnp.float32)
            * score_scale
        )
        grad_values = jnp.einsum(
            "hqk,qhd->khd",
            attn_weights.astype(jnp.bfloat16),
            grad_heads,
            preferred_element_type=jnp.float32,
        )
        return jnp.concatenate(
            [
                grad_keys.reshape(block_len, model_width),
                grad_values.reshape(block_len, model_width),
            ],
            1,
        )

    def query_term(grad_scores, key_block):
        return (
            jnp.einsum("hqk,khd->qhd", grad_scores, key_block, preferred_element_type=jnp.float32)
            * score_scale
        )

    group_rows = group_graphs.shape[0]

    def add_piece(carried, kv_piece, first_row):
        key_piece, value_piece = kv_piece
        piece_rows = key_piece.shape[0]
        block_len = block_length(piece_rows, BLOCK_CAP)

        def add_block(block_state, block_index):
            grad_query, buffer = block_state
            block_start = block_index * block_len
            key_block = lax.dynamic_slice_in_dim(key_piece, block_start, block_len, 0).reshape(
                block_len, HEADS, HEAD_DIM
            )
            value_block = lax.dynamic_slice_in_dim(value_piece, block_start, block_len, 0).reshape(
                block_len, HEADS, HEAD_DIM
            )
            place = first_row + block_start
            key_graphs = lax.dynamic_slice_in_dim(group_graphs, place, block_len, 0)
            attn_weights, grad_scores = score_block(key_block, value_block, key_graphs)
            grad_query = grad_query + query_term(grad_scores, key_block)
            block_terms = key_terms(attn_weights, grad_scores, block_len)
            current = lax.dynamic_slice_in_dim(buffer, place, block_len, 0)
            buffer = lax.dynamic_update_slice_in_dim(buffer, current + block_terms, place, 0)
            return ((grad_query, buffer), None)

        carried, _ = lax.scan(add_block, carried, jnp.arange(piece_rows // block_len))
        return carried

    start_state = (
        jnp.zeros((row_count, HEADS, HEAD_DIM), jnp.float32),
        jnp.zeros((group_rows, 2 * model_width), jnp.float32),
    )
    grad_query, buffer = add_piece(
        start_state,
        (
            lax.all_gather(key_rows, "nodes", axis=0, tiled=True),
            lax.all_gather(value_rows, "nodes", axis=0, tiled=True),
        ),
        jnp.int32(0),
    )
    grad_kv = lax.psum_scatter(buffer, "nodes", scatter_dimension=0, tiled=True)
    return (
        grad_query.reshape(row_count, model_width),
        grad_kv[:, :model_width],
        grad_kv[:, model_width:],
    )


def layer_forward(
    hidden, params, edge_feat, edge_src, edge_dst, halo_send, local_graphs, group_graphs, node_total
):
    w_proj, w_edge, w_qkv, w_out, w_up, w_down, norm_gains, norm_shifts = params
    row_count, model_width = hidden.shape
    hidden_low = hidden.astype(jnp.bfloat16)
    projected = forward_product(hidden_low, w_proj)
    self_term = projected[:, :model_width]
    dest_term = projected[:, 2 * model_width : 3 * model_width]
    source_rows = jnp.concatenate(
        [projected[:, model_width : 2 * model_width], projected[:, 3 * model_width :]], 1
    ).astype(jnp.bfloat16)
    incoming = exchange_sources(source_rows[halo_send])
    extended = jnp.concatenate([source_rows, incoming], 0)
    edge_rows = extended[edge_src].astype(jnp.float32)
    source_b = edge_rows[:, :model_width]
    source_e = edge_rows[:, model_width:]
    edge_proj = forward_product(edge_feat, w_edge)
    gating = jax.nn.sigmoid(dest_term[edge_dst] + source_e + edge_proj)
    numerator = jax.ops.segment_sum(gating * source_b, edge_dst, row_count)
    denominator = jax.ops.segment_sum(gating, edge_dst, row_count)
    message = self_term + numerator / (denominator + GATE_EPS)
    normed_one, standard_one, inv_one = normalize(
        message, norm_gains[0], norm_shifts[0], node_total
    )
    local_out = hidden + jax.nn.silu(normed_one)
    qkv_low = forward_product(hidden_low, w_qkv).astype(jnp.bfloat16)
    query_rows = qkv_low[:, :model_width]
    key_rows = qkv_low[:, model_width : 2 * model_width]
    value_rows = qkv_low[:, 2 * model_width :]
    attn_raw, log_sum = attend_forward(query_rows, key_rows, value_rows, local_graphs, group_graphs)
    attn_low = attn_raw.reshape(row_count, model_width).astype(jnp.bfloat16)
    attn_proj = forward_product(attn_low, w_out)
    normed_two, standard_two, inv_two = normalize(
        hidden + attn_proj, norm_gains[1], norm_shifts[1], node_total
    )
    mixed = local_out + normed_two
    mixed_low = mixed.astype(jnp.bfloat16)
    up_proj = forward_product(mixed_low, w_up)
    activated = jax.nn.silu(up_proj).astype(jnp.bfloat16)
    down_proj = forward_product(activated, w_down)
    normed_three, standard_three, inv_three = normalize(
        mixed + down_proj, norm_gains[2], norm_shifts[2], node_total
    )
    saved = (
        hidden_low,
        source_b,
        gating,
        numerator,
        denominator,
        normed_one,
        standard_one,
        inv_one,
        query_rows,
        key_rows,
        value_rows,
        attn_raw,
        log_sum,
        attn_low,
        standard_two,
        inv_two,
        mixed_low,
        up_proj,
        activated,
        standard_three,
        inv_three,
    )
    return (normed_three, saved)


def layer_backward(
    grad_out,
    params,
    saved,
    edge_feat,
    edge_src,
    edge_dst,
    halo_send,
    local_graphs,
    group_graphs,
    node_total,
):
    w_proj, w_edge, w_qkv, w_out, w_up, w_down, norm_gains, norm_shifts = params
    (
        hidden_low,
        source_b,
        gating,
        numerator,
        denominator,
        normed_one,
        standard_one,
        inv_one,
        query_rows,
        key_rows,
        value_rows,
        attn_raw,
        log_sum,
        attn_low,
        standard_two,
        inv_two,
        mixed_low,
        up_proj,
        activated,
        standard_three,
        inv_three,
    ) = saved
    row_count, model_width = grad_out.shape
    grad_three, gain_three, shift_three = normalize_back(
        grad_out, standard_three, inv_three, norm_gains[2], node_total
    )
    down_grad = grad_three.astype(jnp.bfloat16)
    grad_w_down = outer_product(activated, down_grad)
    up_grad = (times_transposed(down_grad, w_down) * silu_slope_plain(up_proj)).astype(jnp.bfloat16)
    grad_w_up = outer_product(mixed_low, up_grad)
    grad_mixed = grad_three + times_transposed(up_grad, w_up)
    grad_two, gain_two, shift_two = normalize_back(
        grad_mixed, standard_two, inv_two, norm_gains[1], node_total
    )
    out_grad = grad_two.astype(jnp.bfloat16)
    grad_w_out = outer_product(attn_low, out_grad)
    attn_grad = times_transposed(out_grad, w_out).astype(jnp.bfloat16)
    grad_query, grad_key, grad_value = attend_backward(
        query_rows, key_rows, value_rows, attn_grad, attn_raw, log_sum, local_graphs, group_graphs
    )
    qkv_grad = jnp.concatenate([grad_query, grad_key, grad_value], 1).astype(jnp.bfloat16)
    grad_w_qkv = outer_product(hidden_low, qkv_grad)
    grad_message, gain_one, shift_one = normalize_back(
        grad_mixed * silu_slope_plain(normed_one), standard_one, inv_one, norm_gains[0], node_total
    )
    shifted = denominator + GATE_EPS
    grad_numer = grad_message / shifted
    grad_denom = -grad_message * numerator / (shifted * shifted)
    numer_edge = grad_numer[edge_dst]
    grad_gate = numer_edge * source_b + grad_denom[edge_dst]
    grad_pre_edge = grad_gate * gating * (1.0 - gating)
    edge_grad = grad_pre_edge.astype(jnp.bfloat16)
    grad_w_edge = outer_product(edge_feat, edge_grad)
    grad_dest = jax.ops.segment_sum(grad_pre_edge, edge_dst, row_count)
    grad_extended = jax.ops.segment_sum(
        jnp.concatenate([numer_edge * gating, grad_pre_edge], 1),
        edge_src,
        row_count + halo_send.shape[0],
    )
    returned = return_sources(grad_extended[row_count:])
    grad_source = grad_extended[:row_count].at[halo_send].add(returned)
    proj_grad = jnp.concatenate(
        [grad_message, grad_source[:, :model_width], grad_dest, grad_source[:, model_width:]], 1
    ).astype(jnp.bfloat16)
    grad_w_proj = outer_product(hidden_low, proj_grad)
    grad_hidden = (
        grad_mixed
        + grad_two
        + times_transposed(proj_grad, w_proj)
        + times_transposed(qkv_grad, w_qkv)
    )
    weight_grads = (grad_w_proj, grad_w_edge, grad_w_qkv, grad_w_out, grad_w_up, grad_w_down)
    return (
        grad_hidden,
        weight_grads,
        jnp.stack([gain_one, gain_two, gain_three]),
        jnp.stack([shift_one, shift_two, shift_three]),
    )


def per_device(
    node_input,
    edge_feat,
    graph_ids,
    edge_src,
    edge_dst,
    halo_send,
    w_proj,
    w_edge,
    w_qkv,
    w_out,
    w_up,
    w_down,
    norm_gain,
    norm_shift,
    cotangent,
):
    group_graphs = lax.all_gather(graph_ids, "nodes", axis=0, tiled=True)
    node_total = node_input.shape[0] * lax.axis_size("nodes") * lax.axis_size("rep")
    layer_count = w_proj.shape[0]
    layer_params = [
        (
            w_proj[layer_index],
            w_edge[layer_index],
            w_qkv[layer_index],
            w_out[layer_index],
            w_up[layer_index],
            w_down[layer_index],
            norm_gain[layer_index],
            norm_shift[layer_index],
        )
        for layer_index in range(layer_count)
    ]
    hidden = node_input.astype(jnp.float32)
    saved_all = []
    for layer_index in range(layer_count):
        hidden, saved = layer_forward(
            hidden,
            layer_params[layer_index],
            edge_feat,
            edge_src,
            edge_dst,
            halo_send,
            graph_ids,
            group_graphs,
            node_total,
        )
        saved_all.append(saved)
    grad_hidden = cotangent.astype(jnp.float32)
    weight_parts = [None] * layer_count
    gain_parts = [None] * layer_count
    shift_parts = [None] * layer_count
    for layer_index in range(layer_count - 1, -1, -1):
        (
            grad_hidden,
            weight_parts[layer_index],
            gain_parts[layer_index],
            shift_parts[layer_index],
        ) = layer_backward(
            grad_hidden,
            layer_params[layer_index],
            saved_all[layer_index],
            edge_feat,
            edge_src,
            edge_dst,
            halo_send,
            graph_ids,
            group_graphs,
            node_total,
        )
    proj_local = jnp.stack([weight_parts[layer_index][0] for layer_index in range(layer_count)])
    edge_local = jnp.stack([weight_parts[layer_index][1] for layer_index in range(layer_count)])
    qkv_local = jnp.stack([weight_parts[layer_index][2] for layer_index in range(layer_count)])
    out_local = jnp.stack([weight_parts[layer_index][3] for layer_index in range(layer_count)])
    up_local = jnp.stack([weight_parts[layer_index][4] for layer_index in range(layer_count)])
    down_local = jnp.stack([weight_parts[layer_index][5] for layer_index in range(layer_count)])
    grad_proj, grad_edge, grad_qkv, grad_out, grad_up, grad_down = lax.psum(
        (proj_local, edge_local, qkv_local, out_local, up_local, down_local), ("nodes", "rep")
    )
    return (
        hidden,
        grad_hidden,
        grad_proj,
        grad_edge,
        grad_qkv,
        grad_out,
        grad_up,
        grad_down,
        jnp.stack(gain_parts),
        jnp.stack(shift_parts),
    )


def solution(mesh):
    in_specs = (
        P(("rep", "nodes"), None),
        P(("rep", "nodes"), None),
        P(("rep", "nodes")),
        P(("rep", "nodes")),
        P(("rep", "nodes")),
        P(("rep", "nodes")),
        P(),
        P(),
        P(),
        P(),
        P(),
        P(),
        P(),
        P(),
        P(("rep", "nodes"), None),
    )
    out_specs = (
        P(("rep", "nodes"), None),
        P(("rep", "nodes"), None),
        P(),
        P(),
        P(),
        P(),
        P(),
        P(),
        P(),
        P(),
    )
    N, M = mesh.shape["nodes"], mesh.shape["rep"]
    fused = N in (4, 8) and M % 2 == 0 and 512 % (16 * N * M) == 0
    return jax.shard_map(
        functools.partial(fused_device, N, M) if fused else per_device,
        mesh=mesh, in_specs=in_specs, out_specs=out_specs, check_vma=False,
    )
```

```python
import functools
import math

import jax
import jax.numpy as jnp
from jax import lax
from jax.experimental import pallas as pl
from jax.experimental.pallas import tpu as pltpu
from jax.sharding import PartitionSpec as P

HEADS = 8
HEAD_DIM = 32
NEG = -1e30
NORM_EPS = 1e-05
GATE_EPS = 1e-06
F32, BF16, I32 = jnp.float32, jnp.bfloat16, jnp.int32
MESH = pl.DeviceIdType.MESH
SYNCS = 12
STRIP = 32
GROUPS = (
    ("early", 1, 0, 2560, ("core", "y", "nodes")),
    ("conv", 1, 0, 2560, ("core", "y", "nodes")),
    ("qkv", 1, 0, 1536, ("core", "y", "nodes")),
    ("early", 0, 0, 2560, ("core", "x", "y", "z")),
    ("conv", 0, 0, 2560, ("core", "y", "nodes")),
    ("qkv", 0, 0, 1024, ("rep", "nodes")),
    ("qkv", 0, 1024, 512, ("nodes", "rep")),
)


def dot(left, right):
    return lax.dot_general(
        left, right, (((1,), (0,)), ((), ())), preferred_element_type=F32
    )


def dot_nt(left, right):
    return lax.dot_general(
        left, right, (((1,), (1,)), ((), ())), preferred_element_type=F32
    )


def dot_tn(left, right):
    return lax.dot_general(
        left, right, (((0,), (0,)), ((), ())), preferred_element_type=F32
    )


def split(value):
    high = value.astype(BF16)
    return high, (value - high.astype(F32)).astype(BF16)


def sigmoid(value):
    return jax.nn.sigmoid(value)


def silu_slope(value):
    logistic = sigmoid(value)
    return logistic * (1.0 + value * (1.0 - logistic))


def col_sum(value):
    return jnp.sum(value, axis=0, keepdims=True)


def pack(first, second):
    return jnp.concatenate([first[:, :128], first[:, 128:], second[:, :128], second[:, 128:]], 0)


def unpack(tile):
    return [jnp.concatenate([tile[i : i + 1], tile[i + 1 : i + 2]], 1) for i in (0, 2)]


def combine_moments(tiles, count):
    mean = jnp.mean(tiles[:, 0:2], 0)
    off = tiles[:, 0:2] - mean
    return jnp.concatenate([mean, jnp.sum(tiles[:, 2:4] + count * off * off, 0)], 0)


class Refs:
    pass


def axis_sizes(N, M):
    return dict(core=2, y=M // 2, x=2, z=N // 2, rep=M, nodes=N)


def scratch_list(N, M, L, R, E):
    NZ, NB, G = N // 2, N // 4, N * R
    D, FF, W, HH = 256, 512, 4 * R, HEADS // 2 * R
    dma = lambda *shape: pltpu.SemaphoreType.DMA(shape)
    vm = lambda dtype, *shape: pltpu.VMEM(shape, dtype)
    names = dict(
        gb=vm(BF16, L, N, R, D),
        xs=vm(BF16, L, N, R, D),
        meta=vm(I32, N, 8, 256),
        cot=vm(BF16, R, D),
        wp=vm(BF16, L, D, 4 * D),
        we=vm(BF16, L, D, D),
        wqkv=vm(BF16, L, D, 3 * D),
        wo=vm(BF16, L, D, D),
        wu=vm(BF16, L, D, FF),
        wd=vm(BF16, L, FF, D),
        st1=vm(F32, SYNCS, M * N, 4, 128),
        gain=vm(F32, L, 8, D),
        shift=vm(F32, L, 8, D),
        ggain=vm(F32, L, 8, D),
        gshift=vm(F32, L, 8, D),
        iv=vm(F32, L, 8, D),
        moff=vm(F32, N, 8, D),
        move=vm(F32, 8, D),
        le=vm(BF16, E, 1024),
        re=vm(BF16, 1024, D),
        TT=vm(BF16, R, 2 * E),
        ST=vm(BF16, 256, E),
        efT=vm(BF16, D, E),
        HS=vm(BF16, 64, R),
        hx=vm(BF16, L, 64, D),
        A=vm(BF16, R, 64),
        bias=vm(F32, R, G),
        xf=vm(F32, L + 1, R, D),
        xe=vm(BF16, L, 256, D),
        xeT=vm(BF16, D, 256),
        gate=vm(F32, L, E, D),
        bs=vm(BF16, L, E, D),
        num=vm(F32, L, R, D),
        den=vm(F32, L, R, D),
        z0=vm(F32, L, R, D),
        z1=vm(F32, L, R, D),
        z2=vm(F32, L, R, D),
        wkvT=vm(BF16, L, 2 * D, D),
        kvT=vm(BF16, L, 2 * D, G),
        odT=vm(F32, NB, D, R),
        ldT=vm(F32, NB, D, R),
        md=vm(F32, NB, R, D),
        rb=vm(F32, L, NB, R, D),
        pst=vm(BF16, L, HEADS * R, G),
        oraw=vm(F32, L, R, D),
        ob=vm(BF16, L, R, D),
        mb=vm(BF16, L, R, D),
        u=vm(F32, L, R, FF),
        g=vm(BF16, L, R, FF),
        dy=vm(F32, R, D),
        dmix=vm(F32, R, D),
        gy0=vm(F32, R, D),
        local=vm(F32, R, D),
        dxo=vm(F32, R, D),
        dob=vm(F32, R, D),
        dqT=vm(F32, D, R),
        qm=vm(BF16, L, 2, HH, 128),
        q=vm(BF16, L, R, D),
        qT=vm(BF16, D, R),
        dosT=vm(BF16, 128, R),
        dom=vm(BF16, HH, 256),
        sc=vm(F32, 2, max(2 * R, E), W),
        tp=vm(F32, HEADS // 2, R, 128),
        dss=vm(BF16, HH, W),
        dkv=vm(BF16, 2 * D, W),
        gkv=vm(F32, 2 * D, D),
        gg=vm(BF16, 2 * E, 2 * D),
        dn=vm(BF16, 512, 2 * D),
        dproj=vm(BF16, 256, 4 * D),
        dxs=vm(BF16, L, NZ, 2, R, D),
        rs1=vm(BF16, L, NZ, R, D),
        cs=vm(BF16, L, NZ, R, D),
        rs2=vm(BF16, L, NZ, R, D),
        ro=vm(BF16, L, 3, R, D),
        hs=vm(BF16, L, 2, 32, D),
        hr=vm(BF16, L, 2, 32, D),
    )
    names.update(
        gs_early=vm(BF16, L, 2560, 128),
        gs_conv=vm(BF16, L, 2560, 128),
        gs_qkv=vm(BF16, L, 1536, 128),
    )
    sizes = axis_sizes(N, M)
    for g, (_, _, _, rows, stages) in enumerate(GROUPS):
        names[f"go{g}"] = vm(BF16, rows, 128)
        left = rows
        for k, axis in enumerate(stages):
            left //= sizes[axis]
            names[f"ga{g}_{k}"] = vm(BF16, sizes[axis] - 1, left, 128)
            if k < len(stages) - 1:
                names[f"gh{g}_{k}"] = vm(BF16, left, 128)
    names.update(
        ar_s=dma(len(GROUPS)),
        ar_r=dma(sum(2 * len(stages) for *_, stages in GROUPS)),
        ar_l=dma(len(GROUPS)),
        load=dma(9),
        store=dma(2),
        meta_s=dma(1),
        meta_r=dma(1),
        st_s=dma(1),
        st_r=dma(SYNCS),
        ag_s=dma(1),
        agn_r=dma(L),
        agc_r=dma(L, NZ),
        agp_r=dma(L),
        rs_s=dma(1),
        rsp_r=dma(L, NB, 2),
        ro_r=dma(L),
        rsc_r=dma(L),
        hx_s=dma(1),
        hx_r=dma(L),
        hal_s=dma(1),
        hal_r=dma(L),
    )
    return names


IN_NAMES = (
    "x_in", "ids", "edge_src", "edge_dst", "halo", "ef_h", "wp_h", "we_h", "wqkv_h", "wo_h", "wu_h", "wd_h",
    "gain_in", "shift_in", "cot_h",
)
OUT_NAMES = ("out_act", "grad_in", *(f"gout{g}" for g in range(len(GROUPS))), "ggain_out", "gshift_out")


def kernel(N, M, L, names, *args):
    r_ = Refs()
    for name, ref in zip(IN_NAMES + OUT_NAMES + tuple(names), args, strict=True):
        setattr(r_, name, ref)
    R, D = r_.x_in.shape
    E = r_.ef_h.shape[0]
    NZ, NB, G, W = N // 2, N // 4, N * R, 4 * R
    HK = HEADS // 2
    total = float(N * M * R)
    scale = HEAD_DIM ** -0.5
    me = lax.axis_index("nodes")
    rep = lax.axis_index("rep")
    z = me // 2
    par = me % 2
    partner = 2 * z + (1 - par)
    prev = (me + N - 1) % N
    nxt = (me + 1) % N
    zh, zl = z // 2, z % 2
    z_to = lambda t: 2 * ((zh + t // 2) % NB) + (zl + t % 2) % 2
    z_from = lambda t: 2 * ((zh + NB - t // 2) % NB) + (zl + t % 2) % 2

    def remote(src, dst, s_sem, r_sem, **where):
        return pltpu.make_async_remote_copy(
            src_ref=src, dst_ref=dst, send_sem=s_sem, recv_sem=r_sem,
            device_id=where, device_id_type=MESH,
        )

    def send(src, dst, s_sem, r_sem, **where):
        remote(src, dst, s_sem, r_sem, **where).start()

    def send_rows(src, dst, rows, s_sem, r_sem, **where):
        pieces = next(p for p in range(1, rows) if rows % (16 * p) == 0 and rows // p <= 128)
        for at in range(0, rows, rows // pieces):
            cut = pl.ds(at, rows // pieces)
            send(src.at[cut], dst.at[cut], s_sem, r_sem, **where)

    def arrive(dst, r_sem):
        remote(dst, dst, r_sem, r_sem, nodes=partner).wait_recv()

    def sent(src, s_sem):
        remote(src, src, s_sem, s_sem, nodes=partner).wait_send()

    def when(condition, *acts):
        if condition:
            for act in acts:
                act()

    loads = [pltpu.make_async_copy(r_.ef_h, r_.le.at[:, D : 2 * D], r_.load.at[0])] + [
        pltpu.make_async_copy(getattr(r_, f"{name}_h"), getattr(r_, name), r_.load.at[1 + i])
        for i, name in enumerate(("we", "wqkv", "wp", "wo", "wu", "wd", "cot"))
    ]
    own_rows = pltpu.make_async_copy(r_.x_in, r_.gb.at[0, me], r_.load.at[8])
    own_rows.start()
    for load in loads:
        load.start()

    barrier = pltpu.get_barrier_semaphore()
    for dr in range(M):
        for d in range(N):
            if dr + d > 0:
                pl.semaphore_signal(barrier, inc=1, device_id={"rep": (rep + dr) % M, "nodes": (me + d) % N},
                                    device_id_type=MESH)
    pl.semaphore_wait(barrier, M * N - 1)

    def gather_start(l):
        mine = r_.gb.at[l, me]
        for t in range(2, NZ):
            send_rows(mine, mine, R, r_.ag_s.at[0], r_.agc_r.at[l, t], nodes=2 * z_to(t) + par)
        send_rows(mine, mine, R, r_.ag_s.at[0], r_.agn_r.at[l], nodes=partner)
        send_rows(mine, mine, R, r_.ag_s.at[0], r_.agn_r.at[l], nodes=2 * z_to(1) + par)
        send_rows(mine, mine, R, r_.ag_s.at[0], r_.agn_r.at[l], nodes=2 * z_to(1) + 1 - par)

    def gather_pass(l, t):
        piece = r_.gb.at[l, 2 * z_from(t) + par]
        arrive(piece, r_.agc_r.at[l, t])
        send_rows(piece, piece, R, r_.ag_s.at[0], r_.agp_r.at[l], nodes=partner)

    def gather_near(l):
        arrive(r_.gb.at[l, 0:3], r_.agn_r.at[l])

    def gather_far(l):
        arrive(r_.gb.at[l, 0 : NZ - 2], r_.agp_r.at[l])

    def sync_start(k, first, second):
        mine = rep * N + me
        r_.st1[k, mine] = pack(first, second)
        for dr in range(M):
            for d in range(N):
                if dr + d > 0:
                    send(r_.st1.at[k, mine], r_.st1.at[k, mine], r_.st_s.at[0], r_.st_r.at[k],
                         rep=(rep + dr) % M, nodes=(me + d) % N)

    def sync_wait(k):
        arrive(r_.st1.at[k, 0 : M * N - 1], r_.st_r.at[k])

    def sync_moments(k):
        sync_wait(k)
        return unpack(combine_moments(r_.st1[k], float(R)))

    def sync_sums(k):
        sync_wait(k)
        return unpack(jnp.sum(r_.st1[k], 0))

    sizes = axis_sizes(N, M)
    core, row = rep % 2, rep // 2
    places = dict(
        core=(core, lambda t: dict(rep=2 * row + t)),
        y=(row, lambda t: dict(rep=2 * t + core)),
        x=(par, lambda t: dict(nodes=2 * z + t)),
        z=(z, lambda t: dict(nodes=2 * t + par)),
        rep=(rep, lambda t: dict(rep=t)),
        nodes=(me, lambda t: dict(nodes=t)),
    )

    def reduce_step(g, step):
        name, layer, first, rows, stages = GROUPS[g]
        K = len(stages)
        base = sum(2 * len(before) for *_, before in GROUPS[:g])
        gs, out = getattr(r_, f"gs_{name}").at[layer, first : first + rows], getattr(r_, f"go{g}")
        count, offset = [rows], [0]
        for axis in stages:
            count.append(count[-1] // sizes[axis])
            offset.append(offset[-1] + places[axis][0] * count[-1])
        take = lambda start, size: pl.ds(pl.multiple_of(start, 16), size)
        if 1 <= step <= K:
            k = step - 1
            got = getattr(r_, f"ga{g}_{k}")
            arrive(got, r_.ar_r.at[base + k])
            held = gs if k == 0 else getattr(r_, f"gh{g}_{k - 1}")
            index = places[stages[k]][0]
            acc = held[take(index * count[k + 1], count[k + 1])].astype(F32)
            for slot in range(sizes[stages[k]] - 1):
                acc = acc + got[slot].astype(F32)
            if step < K:
                getattr(r_, f"gh{g}_{k}")[...] = acc.astype(BF16)
            else:
                out[take(offset[K], count[K])] = acc.astype(BF16)
        elif step > K:
            k = 2 * K - step
            arrive(out.at[0 : (sizes[stages[k]] - 1) * count[k + 1]], r_.ar_r.at[base + step - 1])
        if step < K:
            held = gs if step == 0 else getattr(r_, f"gh{g}_{step - 1}")
            index, device = places[stages[step]]
            size = sizes[stages[step]]
            for d in range(1, size):
                to = (index + d) % size
                send_rows(held.at[take(to * count[step + 1], count[step + 1])], getattr(r_, f"ga{g}_{step}").at[d - 1],
                     count[step + 1], r_.ar_s.at[g], r_.ar_r.at[base + step], **device(to))
        elif step < 2 * K:
            k = 2 * K - 1 - step
            index, device = places[stages[k]]
            size = sizes[stages[k]]
            here = out.at[take(offset[k + 1], count[k + 1])]
            for d in range(1, size):
                send_rows(here, here, count[k + 1], r_.ar_s.at[g], r_.ar_r.at[base + step],
                          **device((index + d) % size))
        else:
            pltpu.make_async_copy(out, getattr(r_, f"gout{g}"), r_.ar_l.at[g]).start()

    def reduce_drain(g):
        name, _, _, rows, _ = GROUPS[g]
        sent(getattr(r_, f"gs_{name}").at[:, 0 : rows - rows // (M * N)], r_.ar_s.at[g])
        pltpu.make_async_copy(getattr(r_, f"go{g}"), getattr(r_, f"gout{g}"), r_.ar_l.at[g]).wait()

    def put(buf, l, at, value):
        rows = value.shape[0]
        for c in range(value.shape[1] // 128):
            buf[l, at : at + rows] = value[:, 128 * c : 128 * (c + 1)].astype(BF16)
            at += rows
        return at

    lane_head = lax.broadcasted_iota(I32, (R, 128), 1) // HEAD_DIM

    def by_head(parts):
        out = parts[0]
        for k in range(1, HK):
            out = jnp.where(lane_head == k, parts[k], out)
        return out

    r_.meta[me] = jnp.full((8, 256), -1, I32)
    r_.meta[me, 0:1, 0:R] = r_.ids[...].reshape(1, R)
    r_.meta[me, 1:2, 0:48] = r_.halo[...].reshape(1, 48)
    for d in range(1, N):
        send(r_.meta.at[me], r_.meta.at[me], r_.meta_s.at[0], r_.meta_r.at[0], nodes=(me + d) % N)
    own_rows.wait()
    gather_start(0)

    src_row = r_.edge_src[...].reshape(1, E)
    src_row = jnp.where(src_row < R + 24, src_row, src_row + 8)
    dst_row = r_.edge_dst[...].reshape(1, E)
    src_col = jnp.broadcast_to(src_row, (128, E)).T[:, 0:1]
    dst_col = jnp.broadcast_to(dst_row, (128, E)).T[:, 0:1]
    as_mask = lambda cond: cond.astype(F32).astype(BF16)
    r_.le[:, 0:256] = as_mask(src_col == lax.broadcasted_iota(I32, (E, 256), 1))
    target = as_mask(dst_col == lax.broadcasted_iota(I32, (E, 256), 1))
    r_.le[:, 512:768] = target
    r_.le[:, 768:1024] = target
    target = as_mask(dst_row == lax.broadcasted_iota(I32, (R, E), 0))
    r_.TT[:, 0:E] = target
    r_.TT[:, E:] = target
    r_.ST[...] = as_mask(src_row == lax.broadcasted_iota(I32, (256, E), 0))
    r_.dn[R:256] = jnp.zeros((256 - R, 2 * D), BF16)
    r_.dn[256 + R : 512] = jnp.zeros((256 - R, 2 * D), BF16)
    r_.dproj[R:256, 0:D] = jnp.zeros((256 - R, D), BF16)
    r_.dproj[R:256, 2 * D : 3 * D] = jnp.zeros((256 - R, D), BF16)
    halo_col = jnp.broadcast_to(r_.meta[me][1:2, 0:128], (128, 128)).T
    hot = (halo_col[0:48, 0:1] == lax.broadcasted_iota(I32, (48, R), 1)).astype(F32)
    pad = jnp.zeros((8, R), F32)
    r_.HS[...] = jnp.concatenate([hot[0:24], pad, hot[24:48], pad], 0).astype(BF16)
    loads[0].wait()
    r_.efT[...] = r_.le[:, D : 2 * D].T
    for l in range(L):
        for k in range(3):
            r_.gain[l, k : k + 1] = r_.gain_in[k, l : l + 1]
            r_.shift[l, k : k + 1] = r_.shift_in[k, l : l + 1]
    r_.xf[0] = r_.gb[0, me].astype(F32)
    r_.moff[...] = jnp.zeros((N, 8, D), F32)
    r_.move[0:1] = jnp.ones((1, D), F32)
    r_.move[1:2] = jnp.zeros((1, D), F32)
    for load in loads[1:]:
        load.wait()
    for l in range(L):
        r_.wkvT[l] = r_.wqkv[l, :, D:].T

    arrive(r_.meta.at[0 : N - 1], r_.meta_r.at[0])
    id_col = jnp.broadcast_to(r_.meta[me][0:1, 0:R], (128, R)).T[:, 0:1]
    id_row = jnp.concatenate(
        [r_.meta[4 * ((zh + NB - j // 4) % NB) + j % 4][0:1, 0:R] for j in range(N)], 1
    )
    r_.bias[...] = jnp.where(id_col == id_row, 0.0, NEG)

    r_.A[...] = as_mask(r_.meta[me][1:2, 0:64] == lax.broadcasted_iota(I32, (R, 64), 0))

    factor_exp = scale * math.log2(math.e)

    def prepare_queries(l):
        q = dot(r_.xs[l, me], r_.wqkv[l, :, :D]).astype(BF16)
        r_.q[l] = q
        q = q.astype(F32)
        for hf in range(2):
            for k in range(HK):
                part = jnp.where(lane_head == k, q[:, 128 * hf : 128 * (hf + 1)], 0.0)
                r_.qm[l, hf, k * R : (k + 1) * R] = part.astype(BF16)

    def head_dims(hf, k, base=0):
        first = base + hf * 128 + k * HEAD_DIM
        return slice(first, first + HEAD_DIM)

    def head_rows(hf, k, count=1):
        return slice((hf * HK + k) * R, (hf * HK + k + count) * R)

    def lane_half(hf):
        return slice(hf * 128, (hf + 1) * 128)

    def half_of(i):
        return (zh + NB - i) % NB, slice(i * W, (i + 1) * W)

    def attention_keys(l, i):
        half, rows = half_of(i)
        x = r_.xs[l, pl.ds(4 * half, 4)].reshape(W, D)
        r_.kvT[l, :, rows] = dot_nt(r_.wkvT[l], x).astype(BF16)

    def attention_heads(l, i, hfs):
        _, rows = half_of(i)
        for hf in hfs:
            lanes = lane_half(hf)
            ones = jnp.ones((HEAD_DIM, W), BF16)
            for c in range(HK // 2):
                r_.sc[c % 2, 0 : 2 * R] = dot(r_.qm[l, hf, 2 * c * R : 2 * (c + 1) * R], r_.kvT[l, lanes, rows])
                for k in range(2):
                    for at in range(0, R, STRIP):
                        s = r_.sc[c % 2, k * R + at : k * R + at + STRIP] + r_.bias[at : at + STRIP, rows]
                        top = jnp.max(s, 1, keepdims=True)
                        e = jnp.exp2((s - top) * factor_exp)
                        r_.tp[2 * c + k, at : at + STRIP] = jnp.broadcast_to(top, (STRIP, 128))
                        first = (hf * HK + 2 * c + k) * R + at
                        r_.pst[l, first : first + STRIP, rows] = e.astype(BF16)
                for k in range(2):
                    h = 2 * c + k
                    left = jnp.concatenate([r_.kvT[l, head_dims(hf, h, D), rows], ones], 0)
                    o = dot_nt(left, r_.pst[l, head_rows(hf, h), rows])
                    r_.odT[i, head_dims(hf, h)] = o[0:HEAD_DIM]
                    r_.ldT[i, head_dims(hf, h)] = o[HEAD_DIM:]
            r_.md[i, :, lanes] = by_head([r_.tp[k] for k in range(HK)])

    def attention_end(l):
        tops = [r_.md[i].T for i in range(NB)]
        top = tops[0]
        for i in range(1, NB):
            top = jnp.maximum(top, tops[i])
        factors = [jnp.exp2((tops[i] - top) * factor_exp) for i in range(NB)]
        inv = 1.0 / sum(factors[i] * r_.ldT[i] for i in range(NB))
        o = jnp.zeros((D, R), F32)
        for i in range(NB):
            r_.rb[l, i] = (factors[i] * inv).T
            o = o + factors[i] * inv * r_.odT[i]
        o = o.T
        r_.oraw[l] = o
        ob = o.astype(BF16)
        r_.ob[l] = ob
        t1 = r_.xf[l] + dot(ob, r_.wo[l])
        r_.z1[l] = t1
        mean1 = col_sum(t1) / R
        return mean1, col_sum((t1 - mean1) * (t1 - mean1))

    def convolution(l):
        xs = r_.xs
        xb = xs[l, me]
        r_.xe[l, 0:R] = xb
        arrive(r_.xe.at[l, R : R + 64], r_.hx_r.at[l])
        xe = r_.xe[l]
        made = dot(xe, r_.wp[l])
        pd_high, pd_low = split(made[:, 2 * D : 3 * D])
        r_.re[0:256] = made[:, 3 * D :].astype(BF16)
        r_.re[256:512] = r_.we[l]
        r_.re[512:768] = pd_high
        r_.re[768:1024] = pd_low
        r_.gate[l] = dot(r_.le[...], r_.re[...])
        r_.bs[l] = dot(r_.le[:, 0:256], made[:, D : 2 * D].astype(BF16)).astype(BF16)
        for at in range(0, E, 64):
            here = slice(at, at + 64)
            gate = sigmoid(r_.gate[l, here])
            r_.gate[l, here] = gate
            high, low = split(jnp.concatenate([gate * r_.bs[l, here].astype(F32), gate], 1))
            r_.gg[here] = high
            r_.gg[E + at : E + at + 64] = low
        num_den = dot(r_.TT[...], r_.gg[...])
        pa, num, den = made[0:R, 0:D], num_den[:, 0:D], num_den[:, D:]
        r_.num[l] = num
        r_.den[l] = den
        msg = pa + num / (den + GATE_EPS)
        r_.z0[l] = msg
        mean0 = col_sum(msg) / R
        return mean0, col_sum((msg - mean0) * (msg - mean0))

    def forward(l):
        def ready(js):
            for j in js:
                moved = (r_.gb[l, j].astype(F32) + r_.moff[j, 0:1]) * r_.move[0:1] + r_.move[1:2]
                r_.xs[l, j] = moved.astype(BF16)

        r_.xs[l, me] = r_.xf[l].astype(BF16)
        r_.hx[l] = dot(r_.HS[...], r_.xs[l, me]).astype(BF16)
        send(r_.hx.at[l, 0:32], r_.xe.at[l, R + 32 : R + 64], r_.hx_s.at[0], r_.hx_r.at[l], nodes=prev)
        send(r_.hx.at[l, 32:64], r_.xe.at[l, R : R + 32], r_.hx_s.at[0], r_.hx_r.at[l], nodes=nxt)
        prepare_queries(l)
        for t in range(2, NZ):
            gather_pass(l, t)
        mean0, sq0 = convolution(l)
        sync_start(3 * l, mean0, sq0)
        gather_near(l)
        ready([partner, 2 * z_from(1) + par, 2 * z_from(1) + 1 - par])

        attention_keys(l, 0)
        attention_heads(l, 0, (0, 1))
        gather_far(l)
        ready([2 * z_from(t) + p for t in range(2, NZ) for p in range(2)])
        for i in range(1, NB):
            attention_keys(l, i)
            attention_heads(l, i, (0, 1))
        mean1, sq1 = attention_end(l)
        sync_start(3 * l + 1, mean1, sq1)
        mean0, sq0 = sync_moments(3 * l)
        inv0 = lax.rsqrt(sq0 / total + NORM_EPS)
        r_.iv[l, 0:1] = inv0
        z0 = (r_.z0[l] - mean0) * inv0
        r_.z0[l] = z0
        n0 = z0 * r_.gain[l, 0:1] + r_.shift[l, 0:1]
        r_.local[...] = r_.xf[l] + n0 * sigmoid(n0)
        mean1, sq1 = sync_moments(3 * l + 1)
        inv1 = lax.rsqrt(sq1 / total + NORM_EPS)
        r_.iv[l, 1:2] = inv1
        z1 = (r_.z1[l] - mean1) * inv1
        r_.z1[l] = z1
        mix = r_.local[...] + z1 * r_.gain[l, 1:2] + r_.shift[l, 1:2]
        mb = mix.astype(BF16)
        r_.mb[l] = mb
        u = dot(mb, r_.wu[l])
        r_.u[l] = u
        g = (u * sigmoid(u)).astype(BF16)
        r_.g[l] = g
        y = mix + dot(g, r_.wd[l])
        r_.z2[l] = y
        mean = col_sum(y) / R
        cent = y - mean
        k = 3 * l + 2
        sync_start(k, mean, col_sum(cent * cent))

        if l < L - 1:
            r_.gb[l + 1, me] = cent.astype(BF16)
            gather_start(l + 1)

        if l == L - 1:
            dy = r_.cot[...].astype(F32)
            sync_start(3 * L, col_sum(dy), col_sum(dy * cent))

        tot_mean, tot_sq = sync_moments(k)
        inv2 = lax.rsqrt(tot_sq / total + NORM_EPS)
        r_.iv[l, 2:3] = inv2
        z2 = (r_.z2[l] - tot_mean) * inv2
        r_.z2[l] = z2
        gain, shift = r_.gain[l, 2:3], r_.shift[l, 2:3]
        r_.xf[l + 1] = z2 * gain + shift

        if l == L - 1:
            sync_wait(3 * L)
            sums, means = r_.st1[3 * L], r_.st1[k][:, 0:2]
            mean = jnp.mean(means, 0)
            dy_sum = jnp.sum(sums[:, 0:2], 0)
            dy_cent = jnp.sum(sums[:, 2:4] + (means - mean) * sums[:, 0:2], 0)
            dy_sum, dy_cent = unpack(jnp.concatenate([dy_sum, dy_cent], 0))
            r_.gshift[l, 2:3] = dy_sum
            r_.ggain[l, 2:3] = dy_cent * inv2

        for j in range(N):
            tile = r_.st1[k, rep * N + j]
            r_.moff[j, 0:1] = jnp.concatenate([tile[0:1], tile[1:2]], 1) - tot_mean
        r_.move[0:1] = inv2 * gain
        r_.move[1:2] = shift

    for l in range(L):
        forward(l)
    act_copy = pltpu.make_async_copy(r_.xf.at[L], r_.out_act, r_.store.at[0])
    act_copy.start()

    def back_feed_forward(l, k):
        s2, g2 = r_.gshift[l, 2:3], r_.ggain[l, 2:3]
        d3 = r_.gain[l, 2:3] * r_.iv[l, 2:3] * (r_.dy[...] - s2 / total - r_.z2[l] * (g2 / total))
        db = d3.astype(BF16)
        dub = (dot_nt(db, r_.wd[l]) * silu_slope(r_.u[l])).astype(BF16)
        dmix = d3 + dot_nt(dub, r_.wu[l])
        r_.dmix[...] = dmix
        n0 = r_.z0[l] * r_.gain[l, 0:1] + r_.shift[l, 0:1]
        gy0 = dmix * silu_slope(n0)
        sync_start(k, col_sum(dmix), col_sum(dmix * r_.z1[l]))
        sync_start(k + 1, col_sum(gy0), col_sum(gy0 * r_.z0[l]))
        r_.gy0[...] = gy0
        at = put(r_.gs_early, l, 512, dot_tn(r_.mb[l], dub))
        put(r_.gs_early, l, at, dot_tn(r_.g[l], db))
        r_.xeT[...] = r_.xe[l].T
        r_.qT[...] = r_.q[l].T

    def back_norms(l, k):
        s1, g1 = sync_sums(k)
        r_.gshift[l, 1:2] = s1
        r_.ggain[l, 1:2] = g1
        dmix = r_.dmix[...]
        d2 = r_.gain[l, 1:2] * r_.iv[l, 1:2] * (dmix - s1 / total - r_.z1[l] * (g1 / total))
        dab = d2.astype(BF16)
        r_.dxo[...] = dmix + d2
        r_.dob[...] = dot_nt(dab, r_.wo[l]).astype(BF16).astype(F32)
        put(r_.gs_early, l, 0, dot_tn(r_.ob[l], dab))
        r_.gkv[...] = jnp.zeros((2 * D, D), F32)
        r_.dqT[...] = jnp.zeros((D, R), F32)

    def back_half(i):
        t1 = (i + 1) % NB
        half = (zh + t1) % NB
        place = (NB - t1) % NB
        return place, half, slice(place * W, (place + 1) * W)

    def back_heads(l, i, hf):
        place, half, rows = back_half(i)
        if True:
            lanes = lane_half(hf)
            dos = r_.dob[:, lanes] * r_.rb[l, place, :, lanes]
            prod = dos * r_.oraw[l, :, lanes]
            for k in range(HK):
                r_.dom[k * R : (k + 1) * R, 0:128] = jnp.where(lane_head == k, dos, 0.0).astype(BF16)
                r_.dom[k * R : (k + 1) * R, 128:256] = jnp.where(lane_head == k, -prod, 0.0).astype(BF16)
            r_.dosT[...] = dos.T.astype(BF16)
            values = slice(D + hf * 128, D + (hf + 1) * 128)
            right = jnp.concatenate([r_.kvT[l, values, rows], jnp.ones((128, W), BF16)], 0)
            for c in range(HK // 2):
                both = slice(2 * c * R, 2 * (c + 1) * R)
                r_.sc[c % 2, 0 : 2 * R] = dot(r_.dom[both], right)
                for k in range(2):
                    for at in range(0, R, STRIP):
                        first = (hf * HK + 2 * c + k) * R + at
                        e = r_.pst[l, first : first + STRIP, rows].astype(F32)
                        ds = e * r_.sc[c % 2, k * R + at : k * R + at + STRIP]
                        r_.dss[(2 * c + k) * R + at : (2 * c + k) * R + at + STRIP] = ds.astype(BF16)
                for k in range(2):
                    h = 2 * c + k
                    mine, dims = slice(h * R, (h + 1) * R), head_dims(hf, h)
                    r_.dqT[dims] += dot_nt(r_.kvT[l, dims, rows], r_.dss[mine])
                    r_.dkv[dims] = (dot(r_.qT[dims], r_.dss[mine]) * scale).astype(BF16)
                    dv = dot(r_.dosT[h * HEAD_DIM : (h + 1) * HEAD_DIM], r_.pst[l, head_rows(hf, h), rows])
                    r_.dkv[head_dims(hf, h, D)] = dv.astype(BF16)

    def back_rows(l, i):
        _, half, _ = back_half(i)
        dx = dot(r_.wqkv[l, :, D:], r_.dkv[...]).T
        r_.dxs[l, pl.ds(2 * half, 2)] = dx.astype(BF16).reshape(2, 2, R, D)

        if i < NB - 1:
            for t in (2 * (i + 1), 2 * (i + 1) + 1):
                zb = z_to(t)
                send_rows(r_.dxs.at[l, zb, 1 - par], r_.rs1.at[l, zb], R,
                          r_.rs_s.at[0], r_.rsp_r.at[l, i, t % 2], nodes=partner)

        else:
            near = z_to(1)
            send_rows(r_.dxs.at[l, z, 1 - par], r_.ro.at[l, 0], R, r_.rs_s.at[0], r_.ro_r.at[l], nodes=partner)
            send_rows(r_.dxs.at[l, near, par], r_.ro.at[l, 1], R, r_.rs_s.at[0], r_.ro_r.at[l], nodes=2 * near + par)
            send_rows(r_.dxs.at[l, near, 1 - par], r_.ro.at[l, 2], R, r_.rs_s.at[0], r_.ro_r.at[l],
                 nodes=2 * near + 1 - par)

        r_.gkv[...] += dot(r_.dkv[...], r_.xs[l, pl.ds(4 * half, 4)].reshape(W, D))

    def pass_on(l, i, t):
        zb = z_to(t)
        arrive(r_.rs1.at[l, zb], r_.rsp_r.at[l, i, t % 2])
        both = r_.dxs[l, zb, par].astype(F32) + r_.rs1[l, zb].astype(F32)
        r_.cs[l, zb] = both.astype(BF16)
        send_rows(r_.cs.at[l, zb], r_.rs2.at[l, z], R, r_.rs_s.at[0], r_.rsc_r.at[l], nodes=2 * zb + par)

    def back_convolution(l, k):
        s0, g0 = unpack(jnp.sum(r_.st1[k + 1], 0))
        r_.gshift[l, 0:1] = s0
        r_.ggain[l, 0:1] = g0
        inv_den = 1.0 / (r_.den[l] + GATE_EPS)
        dm = r_.gain[l, 0:1] * r_.iv[l, 0:1] * (r_.gy0[...] - s0 / total - r_.z0[l] * (g0 / total))
        dnum = dm * inv_den
        dden = -dnum * r_.num[l] * inv_den
        high, low = split(jnp.concatenate([dnum, dden], 1))
        r_.dn[0:R] = high
        r_.dn[256 : 256 + R] = low
        r_.sc[0, 0:E, 0 : 2 * D] = dot(r_.le[:, 512:1024], r_.dn[...])
        for at in range(0, E, 64):
            here = slice(at, at + 64)
            gate, dnum_e = r_.gate[l, here], r_.sc[0, here, 0:D]
            dgp = (dnum_e * r_.bs[l, here].astype(F32) + r_.sc[0, here, D : 2 * D]) * gate * (1.0 - gate)
            r_.gg[here, 0:D] = (dnum_e * gate).astype(BF16)
            r_.gg[here, D:] = dgp.astype(BF16)
        ext = dot(r_.ST[...], r_.gg[0:E]).astype(BF16)
        r_.dproj[0:R, 0:D] = dm.astype(BF16)
        r_.dproj[:, D : 2 * D] = ext[:, 0:D]
        r_.dproj[0:R, 2 * D : 3 * D] = dot(r_.TT[:, 0:E], r_.gg[0:E, D:]).astype(BF16)
        r_.dproj[:, 3 * D :] = ext[:, D:]
        dxe = dot_nt(r_.dproj[...], r_.wp[l])
        r_.hs[l, 0] = dxe[R : R + 32].astype(BF16)
        r_.hs[l, 1] = dxe[R + 32 : R + 64].astype(BF16)
        r_.dxo[...] += dxe[0:R]

    def send_halo(l):
        send(r_.hs.at[l, 0], r_.hr.at[l, 1], r_.hal_s.at[0], r_.hal_r.at[l], nodes=prev)
        send(r_.hs.at[l, 1], r_.hr.at[l, 0], r_.hal_s.at[0], r_.hal_r.at[l], nodes=nxt)

    def conv_weight_grads(l):
        at = put(r_.gs_conv, l, 0, dot(r_.xeT[...], r_.dproj[...]))
        put(r_.gs_conv, l, at, dot(r_.efT[...], r_.gg[0:E, D:]))

    def back_input(l):
        dx = r_.dxo[...]
        dx = dx + r_.dxs[l, z, par].astype(F32)
        arrive(r_.ro.at[l], r_.ro_r.at[l])
        for slot in range(3):
            dx = dx + r_.ro[l, slot].astype(F32)
        if NZ > 2:
            arrive(r_.rs2.at[l, 0 : NZ - 2], r_.rsc_r.at[l])
        for t in range(2, NZ):
            dx = dx + r_.rs2[l, z_from(t)].astype(F32)
        arrive(r_.hr.at[l], r_.hal_r.at[l])
        back = jnp.concatenate(
            [r_.hr[l, 0].astype(F32)[0:24], r_.hr[l, 1].astype(F32)[0:24], jnp.zeros((16, D), F32)], 0
        )
        return dx + dot(r_.A[...], back.astype(BF16))

    r_.dy[...] = r_.cot[...].astype(F32)

    E1, C1, Q1, E0, C0, QK0, V0 = range(len(GROUPS))

    def steps(*pairs):
        return [functools.partial(reduce_step, g, k) for g, k in pairs]

    r_.dy[...] = r_.cot[...].astype(F32)

    def backward(b):
        l = L - 1 - b
        first, last = b == 0, b == L - 1
        k = 3 * L + 1 + 2 * b
        back_feed_forward(l, k)
        when(last, *steps((E1, 3), (Q1, 2)))
        back_norms(l, k)
        if first:
            when(True, *steps((E1, 0)))
            back_heads(l, 0, 0)
            back_heads(l, 0, 1)
            back_rows(l, 0)
            when(True, *steps((E1, 1)))
            sync_wait(k + 1)
            back_convolution(l, k)
            send_halo(l)
            pass_on(l, 0, 2)
            back_heads(l, 1, 0)
            pass_on(l, 0, 3)
            back_heads(l, 1, 1)
            back_rows(l, 1)
            conv_weight_grads(l)
            when(True, *steps((C1, 0)))
        else:
            when(True, *steps((C1, 3), (E1, 4), (E0, 0)))
            sync_wait(k + 1)
            back_convolution(l, k)
            back_heads(l, 0, 0)
            send_halo(l)
            when(True, *steps((Q1, 3), (E1, 5), (C1, 4), (E0, 1)))
            conv_weight_grads(l)
            back_heads(l, 0, 1)
            back_rows(l, 0)
            when(True, *steps((C0, 0), (E0, 2), (Q1, 4), (E1, 6), (C1, 5)))
            back_heads(l, 1, 0)
            when(True, *steps((C0, 1), (E0, 3), (Q1, 5), (C1, 6)))
            for t in range(2, NZ):
                pass_on(l, 0, t)
            back_heads(l, 1, 1)
            back_rows(l, 1)
            when(True, *steps((C0, 2), (E0, 4), (Q1, 6)))
        dqb = (r_.dqT[...].T * scale).astype(BF16)
        r_.dxo[...] += dot_nt(dqb, r_.wqkv[l, :, 0:D])
        at = put(r_.gs_qkv, l, 0, dot(r_.xeT[:, 0:R], dqb))
        put(r_.gs_qkv, l, at, r_.gkv[...].T)
        if first:
            when(True, *steps((Q1, 0), (C1, 1)))
            dx = back_input(l)
            r_.dy[...] = dx
            below = L - 2
            sync_start(SYNCS - 1, col_sum(dx), col_sum(dx * r_.z2[below]))
            when(True, *steps((E1, 2), (Q1, 1)))
            s2, g2 = sync_sums(SYNCS - 1)
            r_.gshift[below, 2:3] = s2
            r_.ggain[below, 2:3] = g2
            when(True, *steps((C1, 2)))

    for b in range(L):
        backward(b)
    for step in steps((QK0, 0), (V0, 0), (E0, 5), (C0, 3), (V0, 1), (QK0, 1)):
        step()
    r_.dy[...] = back_input(0)
    in_copy = pltpu.make_async_copy(r_.dy, r_.grad_in, r_.store.at[1])
    in_copy.start()
    for step in steps(
        (E0, 6), (C0, 4), (V0, 2), (QK0, 2),
        (E0, 7), (C0, 5), (V0, 3), (QK0, 3),
        (E0, 8), (C0, 6), (V0, 4), (QK0, 4),
    ):
        step()
    for l in range(L):
        for k in range(3):
            r_.ggain_out[k, l : l + 1] = r_.ggain[l, k : k + 1]
            r_.gshift_out[k, l : l + 1] = r_.gshift[l, k : k + 1]
    for g in range(len(GROUPS)):
        reduce_drain(g)
    sent(r_.meta.at[0 : N - 1], r_.meta_s.at[0])
    sent(r_.st1.at[:, 0 : M * N - 1], r_.st_s.at[0])
    sent(r_.gb.at[:, 0 : 3 + 2 * (NZ - 2)], r_.ag_s.at[0])
    sent(r_.gb.at[:, 0 : 2 * (NB - 1) + 3 + NZ - 2], r_.rs_s.at[0])
    sent(r_.hs, r_.hal_s.at[0])
    sent(r_.hx, r_.hx_s.at[0])
    act_copy.wait()
    in_copy.wait()


def finish_kernel(act_h, gin_h, *refs):
    n = len(GROUPS)
    held, (ggain_h, gshift_h), refs = refs[:n], refs[n : n + 2], refs[n + 2 :]
    act_o, gin_o, proj_o, edge_o, qkv_o, out_o, up_o, down_o, ggain_o, gshift_o = refs[:10]
    summed, refs = refs[10 : 10 + n], refs[10 + n :]
    act, gin, proj, edge, qkv, out, up, down, in_sem, out_sem = refs
    loads = [
        pltpu.make_async_copy(src, dst, in_sem.at[i])
        for i, (src, dst) in enumerate(zip(held + (act_h, gin_h), summed + (act, gin), strict=True))
    ]
    for load in loads:
        load.start()
    ggain_o[...] = ggain_h[...]
    gshift_o[...] = gshift_h[...]
    stores = []

    def store(src, dst):
        copy = pltpu.make_async_copy(src, dst, out_sem.at[len(stores)])
        copy.start()
        stores.append(copy)

    def widen(dst, l, g, at, first=0, last=None):
        rows = dst.shape[1]
        for c in range(first, dst.shape[2] // 128 if last is None else last):
            dst[l, :, 128 * c : 128 * (c + 1)] = summed[g][at : at + rows].astype(F32)
            at += rows
        return at

    for g, (name, l, first, rows, _) in enumerate(GROUPS):
        loads[g].wait()
        if name == "early":
            at = widen(out, l, g, 0)
            store(out.at[l], out_o.at[l])
            at = widen(up, l, g, at)
            store(up.at[l], up_o.at[l])
            widen(down, l, g, at)
            store(down.at[l], down_o.at[l])
        elif name == "conv":
            at = widen(proj, l, g, 0)
            store(proj.at[l], proj_o.at[l])
            widen(edge, l, g, at)
            store(edge.at[l], edge_o.at[l])
        else:
            widen(qkv, l, g, 0, first // 256, (first + rows) // 256)
            if first + rows == 1536:
                store(qkv.at[l], qkv_o.at[l])
    for i, (src, dst) in enumerate(((act, act_o), (gin, gin_o))):
        loads[n + i].wait()
        store(src, dst)
    for copy in stores:
        copy.wait()


def fused_device(
    N, M, node_input, edge_feat, graph_ids, edge_src, edge_dst, halo_send, w_proj, w_edge, w_qkv,
    w_out, w_up, w_down, norm_gain, norm_shift, cotangent,
):
    R, D = node_input.shape
    E = edge_feat.shape[0]
    L = w_proj.shape[0]
    names = scratch_list(N, M, L, R, E)
    vmem = pl.BlockSpec(memory_space=pltpu.VMEM)
    hbm = pl.BlockSpec(memory_space=pltpu.HBM)
    shape = jax.ShapeDtypeStruct
    rows = shape((R, D), F32)
    norm = shape((3, L, D), F32)
    groups = [shape((rows_g, 128), BF16) for _, _, _, rows_g, _ in GROUPS]
    outs = pl.pallas_call(
        functools.partial(kernel, N, M, L, tuple(names)),
        out_shape=[rows, rows, *groups, norm, norm],
        in_specs=[hbm] + [vmem] * 4 + [hbm] * 7 + [vmem] * 2 + [hbm],
        out_specs=[hbm] * (2 + len(GROUPS)) + [vmem] * 2,
        scratch_shapes=list(names.values()),
        compiler_params=pltpu.CompilerParams(
            collective_id=0, has_side_effects=True, vmem_limit_bytes=60 << 20
        ),
        name="layers",
    )(node_input, graph_ids, edge_src, edge_dst, halo_send, edge_feat, w_proj, w_edge, w_qkv, w_out, w_up,
      w_down, norm_gain.transpose(1, 0, 2), norm_shift.transpose(1, 0, 2), cotangent)
    weights = [shape(w.shape, F32) for w in (w_proj, w_edge, w_qkv, w_out, w_up, w_down)]
    results = pl.pallas_call(
        finish_kernel,
        out_shape=[rows, rows, *weights, norm, norm],
        in_specs=[hbm] * (2 + len(GROUPS)) + [vmem] * 2,
        out_specs=[hbm] * 8 + [vmem] * 2,
        scratch_shapes=[pltpu.VMEM(s.shape, s.dtype) for s in (*groups, rows, rows, *weights)]
        + [pltpu.SemaphoreType.DMA((len(GROUPS) + 2,)), pltpu.SemaphoreType.DMA((14,))],
        compiler_params=pltpu.CompilerParams(vmem_limit_bytes=60 << 20),
        name="gradients",
    )(*outs)
    ggain, gshift = results[8].transpose(1, 0, 2), results[9].transpose(1, 0, 2)
    return (*results[:8], ggain, gshift)


BLOCK_CAP = 2048


def extended_2(block, sides, width):
    for axis, dim in sides:
        count = lax.axis_size(axis)
        forward = [(i, i + 1) for i in range(count - 1)]
        forward.append((count - 1, 0))
        backward = [(target, source) for source, target in forward]
        low = lax.ppermute(
            lax.slice_in_dim(block, block.shape[dim] - width, None, axis=dim), axis, forward
        )
        high = lax.ppermute(lax.slice_in_dim(block, 0, width, axis=dim), axis, backward)
        block = jnp.concatenate([low, block, high], axis=dim)
    return block


def block_length(total_rows, upper_limit):
    for length in range(min(total_rows, upper_limit), 0, -1):
        if total_rows % length == 0:
            return length
    return 1


def outer_product(left, right):
    return lax.dot_general(
        left, right, (((0,), (0,)), ((), ())), preferred_element_type=jnp.float32
    )


def times_transposed(left, weight):
    return lax.dot_general(
        left, weight, (((1,), (1,)), ((), ())), preferred_element_type=jnp.float32
    )


def forward_product(left, weight):
    return jnp.dot(left, weight, preferred_element_type=jnp.float32)


def silu_slope_plain(inputs):
    logistic = jax.nn.sigmoid(inputs)
    return logistic * (1.0 + inputs * (1.0 - logistic))


def normalize(inputs, gain_row, shift_row, node_total):
    batch_mean = lax.psum(jnp.sum(inputs, 0), ("nodes", "rep")) / node_total
    centred = inputs - batch_mean
    batch_var = lax.psum(jnp.sum(centred * centred, 0), ("nodes", "rep")) / node_total
    inv_std = lax.rsqrt(batch_var + NORM_EPS)
    standard = (inputs - batch_mean) * inv_std
    return (standard * gain_row + shift_row, standard, inv_std)


def normalize_back(grad_out, standard, inv_std, gain_row, node_total):
    shift_grad, gain_grad = lax.psum(
        (jnp.sum(grad_out, 0), jnp.sum(grad_out * standard, 0)), ("nodes", "rep")
    )
    grad_in = (
        gain_row
        * inv_std
        * (grad_out - shift_grad / node_total - standard * gain_grad / node_total)
    )
    return (grad_in, gain_grad, shift_grad)


def exchange_sources(outgoing):
    halo_rows = outgoing.shape[0] // 2
    grown = extended_2(outgoing, (("nodes", 0),), halo_rows)
    return jnp.concatenate([grown[:halo_rows], grown[3 * halo_rows :]], 0)


def return_sources(incoming_grad):
    halo_rows = incoming_grad.shape[0] // 2
    grown = extended_2(incoming_grad.astype(jnp.bfloat16), (("nodes", 0),), halo_rows).astype(
        incoming_grad.dtype
    )
    return jnp.concatenate([grown[:halo_rows], grown[3 * halo_rows :]], 0)


def attend_forward(query_rows, key_rows, value_rows, local_graphs, group_graphs):
    row_count = query_rows.shape[0]
    score_scale = HEAD_DIM ** (-0.5)
    queries = query_rows.reshape(row_count, HEADS, HEAD_DIM)

    def add_piece(carried, kv_piece, first_row):
        key_piece, value_piece = kv_piece
        piece_rows = key_piece.shape[0]
        block_len = block_length(piece_rows, BLOCK_CAP)

        def add_block(block_state, block_index):
            row_max, row_sum, accumulated = block_state
            block_start = block_index * block_len
            key_block = lax.dynamic_slice_in_dim(key_piece, block_start, block_len, 0).reshape(
                block_len, HEADS, HEAD_DIM
            )
            value_block = lax.dynamic_slice_in_dim(value_piece, block_start, block_len, 0).reshape(
                block_len, HEADS, HEAD_DIM
            )
            key_graphs = lax.dynamic_slice_in_dim(
                group_graphs, first_row + block_start, block_len, 0
            )
            same_graph = (local_graphs[:, None] == key_graphs[None, :])[None]
            scores = (
                jnp.einsum("qhd,khd->hqk", queries, key_block, preferred_element_type=jnp.float32)
                * score_scale
            )
            scores = jnp.where(same_graph, scores, NEG)
            new_max = jnp.maximum(row_max, jnp.max(scores, 2))
            weights = jnp.where(same_graph, jnp.exp(scores - new_max[:, :, None]), 0.0)
            factor = jnp.exp(row_max - new_max)
            row_sum = row_sum * factor + jnp.sum(weights, 2)
            contrib = jnp.einsum(
                "hqk,khd->qhd",
                weights.astype(jnp.bfloat16),
                value_block,
                preferred_element_type=jnp.float32,
            )
            accumulated = accumulated * jnp.transpose(factor)[:, :, None] + contrib
            return ((new_max, row_sum, accumulated), None)

        carried, _ = lax.scan(add_block, carried, jnp.arange(piece_rows // block_len))
        return carried

    start_state = (
        jnp.full((HEADS, row_count), NEG, jnp.float32),
        jnp.zeros((HEADS, row_count), jnp.float32),
        jnp.zeros((row_count, HEADS, HEAD_DIM), jnp.float32),
    )
    row_max, row_sum, accumulated = add_piece(
        start_state,
        (
            lax.all_gather(key_rows, "nodes", axis=0, tiled=True),
            lax.all_gather(value_rows, "nodes", axis=0, tiled=True),
        ),
        jnp.int32(0),
    )
    attn_raw = accumulated / jnp.transpose(row_sum)[:, :, None]
    log_sum = row_max + jnp.log(row_sum)
    return (attn_raw, log_sum)


def attend_backward(
    query_rows, key_rows, value_rows, grad_low, attn_raw, log_sum, local_graphs, group_graphs
):
    row_count = query_rows.shape[0]
    model_width = HEADS * HEAD_DIM
    score_scale = HEAD_DIM ** (-0.5)
    queries = query_rows.reshape(row_count, HEADS, HEAD_DIM)
    grad_heads = grad_low.reshape(row_count, HEADS, HEAD_DIM)
    row_delta = jnp.einsum("qhd,qhd->hq", grad_heads.astype(jnp.float32), attn_raw)

    def score_block(key_block, value_block, key_graphs):
        same_graph = (local_graphs[:, None] == key_graphs[None, :])[None]
        scores = (
            jnp.einsum("qhd,khd->hqk", queries, key_block, preferred_element_type=jnp.float32)
            * score_scale
        )
        attn_weights = jnp.exp(jnp.where(same_graph, scores - log_sum[:, :, None], NEG))
        grad_weights = jnp.einsum(
            "qhd,khd->hqk", grad_heads, value_block, preferred_element_type=jnp.float32
        )
        grad_scores = (attn_weights * (grad_weights - row_delta[:, :, None])).astype(jnp.bfloat16)
        return (attn_weights, grad_scores)

    def key_terms(attn_weights, grad_scores, block_len):
        grad_keys = (
            jnp.einsum("hqk,qhd->khd", grad_scores, queries, preferred_element_type=jnp.float32)
            * score_scale
        )
        grad_values = jnp.einsum(
            "hqk,qhd->khd",
            attn_weights.astype(jnp.bfloat16),
            grad_heads,
            preferred_element_type=jnp.float32,
        )
        return jnp.concatenate(
            [
                grad_keys.reshape(block_len, model_width),
                grad_values.reshape(block_len, model_width),
            ],
            1,
        )

    def query_term(grad_scores, key_block):
        return (
            jnp.einsum("hqk,khd->qhd", grad_scores, key_block, preferred_element_type=jnp.float32)
            * score_scale
        )

    group_rows = group_graphs.shape[0]

    def add_piece(carried, kv_piece, first_row):
        key_piece, value_piece = kv_piece
        piece_rows = key_piece.shape[0]
        block_len = block_length(piece_rows, BLOCK_CAP)

        def add_block(block_state, block_index):
            grad_query, buffer = block_state
            block_start = block_index * block_len
            key_block = lax.dynamic_slice_in_dim(key_piece, block_start, block_len, 0).reshape(
                block_len, HEADS, HEAD_DIM
            )
            value_block = lax.dynamic_slice_in_dim(value_piece, block_start, block_len, 0).reshape(
                block_len, HEADS, HEAD_DIM
            )
            place = first_row + block_start
            key_graphs = lax.dynamic_slice_in_dim(group_graphs, place, block_len, 0)
            attn_weights, grad_scores = score_block(key_block, value_block, key_graphs)
            grad_query = grad_query + query_term(grad_scores, key_block)
            block_terms = key_terms(attn_weights, grad_scores, block_len)
            current = lax.dynamic_slice_in_dim(buffer, place, block_len, 0)
            buffer = lax.dynamic_update_slice_in_dim(buffer, current + block_terms, place, 0)
            return ((grad_query, buffer), None)

        carried, _ = lax.scan(add_block, carried, jnp.arange(piece_rows // block_len))
        return carried

    start_state = (
        jnp.zeros((row_count, HEADS, HEAD_DIM), jnp.float32),
        jnp.zeros((group_rows, 2 * model_width), jnp.float32),
    )
    grad_query, buffer = add_piece(
        start_state,
        (
            lax.all_gather(key_rows, "nodes", axis=0, tiled=True),
            lax.all_gather(value_rows, "nodes", axis=0, tiled=True),
        ),
        jnp.int32(0),
    )
    grad_kv = lax.psum_scatter(buffer, "nodes", scatter_dimension=0, tiled=True)
    return (
        grad_query.reshape(row_count, model_width),
        grad_kv[:, :model_width],
        grad_kv[:, model_width:],
    )


def layer_forward(
    hidden, params, edge_feat, edge_src, edge_dst, halo_send, local_graphs, group_graphs, node_total
):
    w_proj, w_edge, w_qkv, w_out, w_up, w_down, norm_gains, norm_shifts = params
    row_count, model_width = hidden.shape
    hidden_low = hidden.astype(jnp.bfloat16)
    projected = forward_product(hidden_low, w_proj)
    self_term = projected[:, :model_width]
    dest_term = projected[:, 2 * model_width : 3 * model_width]
    source_rows = jnp.concatenate(
        [projected[:, model_width : 2 * model_width], projected[:, 3 * model_width :]], 1
    ).astype(jnp.bfloat16)
    incoming = exchange_sources(source_rows[halo_send])
    extended = jnp.concatenate([source_rows, incoming], 0)
    edge_rows = extended[edge_src].astype(jnp.float32)
    source_b = edge_rows[:, :model_width]
    source_e = edge_rows[:, model_width:]
    edge_proj = forward_product(edge_feat, w_edge)
    gating = jax.nn.sigmoid(dest_term[edge_dst] + source_e + edge_proj)
    numerator = jax.ops.segment_sum(gating * source_b, edge_dst, row_count)
    denominator = jax.ops.segment_sum(gating, edge_dst, row_count)
    message = self_term + numerator / (denominator + GATE_EPS)
    normed_one, standard_one, inv_one = normalize(
        message, norm_gains[0], norm_shifts[0], node_total
    )
    local_out = hidden + jax.nn.silu(normed_one)
    qkv_low = forward_product(hidden_low, w_qkv).astype(jnp.bfloat16)
    query_rows = qkv_low[:, :model_width]
    key_rows = qkv_low[:, model_width : 2 * model_width]
    value_rows = qkv_low[:, 2 * model_width :]
    attn_raw, log_sum = attend_forward(query_rows, key_rows, value_rows, local_graphs, group_graphs)
    attn_low = attn_raw.reshape(row_count, model_width).astype(jnp.bfloat16)
    attn_proj = forward_product(attn_low, w_out)
    normed_two, standard_two, inv_two = normalize(
        hidden + attn_proj, norm_gains[1], norm_shifts[1], node_total
    )
    mixed = local_out + normed_two
    mixed_low = mixed.astype(jnp.bfloat16)
    up_proj = forward_product(mixed_low, w_up)
    activated = jax.nn.silu(up_proj).astype(jnp.bfloat16)
    down_proj = forward_product(activated, w_down)
    normed_three, standard_three, inv_three = normalize(
        mixed + down_proj, norm_gains[2], norm_shifts[2], node_total
    )
    saved = (
        hidden_low,
        source_b,
        gating,
        numerator,
        denominator,
        normed_one,
        standard_one,
        inv_one,
        query_rows,
        key_rows,
        value_rows,
        attn_raw,
        log_sum,
        attn_low,
        standard_two,
        inv_two,
        mixed_low,
        up_proj,
        activated,
        standard_three,
        inv_three,
    )
    return (normed_three, saved)


def layer_backward(
    grad_out,
    params,
    saved,
    edge_feat,
    edge_src,
    edge_dst,
    halo_send,
    local_graphs,
    group_graphs,
    node_total,
):
    w_proj, w_edge, w_qkv, w_out, w_up, w_down, norm_gains, norm_shifts = params
    (
        hidden_low,
        source_b,
        gating,
        numerator,
        denominator,
        normed_one,
        standard_one,
        inv_one,
        query_rows,
        key_rows,
        value_rows,
        attn_raw,
        log_sum,
        attn_low,
        standard_two,
        inv_two,
        mixed_low,
        up_proj,
        activated,
        standard_three,
        inv_three,
    ) = saved
    row_count, model_width = grad_out.shape
    grad_three, gain_three, shift_three = normalize_back(
        grad_out, standard_three, inv_three, norm_gains[2], node_total
    )
    down_grad = grad_three.astype(jnp.bfloat16)
    grad_w_down = outer_product(activated, down_grad)
    up_grad = (times_transposed(down_grad, w_down) * silu_slope_plain(up_proj)).astype(jnp.bfloat16)
    grad_w_up = outer_product(mixed_low, up_grad)
    grad_mixed = grad_three + times_transposed(up_grad, w_up)
    grad_two, gain_two, shift_two = normalize_back(
        grad_mixed, standard_two, inv_two, norm_gains[1], node_total
    )
    out_grad = grad_two.astype(jnp.bfloat16)
    grad_w_out = outer_product(attn_low, out_grad)
    attn_grad = times_transposed(out_grad, w_out).astype(jnp.bfloat16)
    grad_query, grad_key, grad_value = attend_backward(
        query_rows, key_rows, value_rows, attn_grad, attn_raw, log_sum, local_graphs, group_graphs
    )
    qkv_grad = jnp.concatenate([grad_query, grad_key, grad_value], 1).astype(jnp.bfloat16)
    grad_w_qkv = outer_product(hidden_low, qkv_grad)
    grad_message, gain_one, shift_one = normalize_back(
        grad_mixed * silu_slope_plain(normed_one), standard_one, inv_one, norm_gains[0], node_total
    )
    shifted = denominator + GATE_EPS
    grad_numer = grad_message / shifted
    grad_denom = -grad_message * numerator / (shifted * shifted)
    numer_edge = grad_numer[edge_dst]
    grad_gate = numer_edge * source_b + grad_denom[edge_dst]
    grad_pre_edge = grad_gate * gating * (1.0 - gating)
    edge_grad = grad_pre_edge.astype(jnp.bfloat16)
    grad_w_edge = outer_product(edge_feat, edge_grad)
    grad_dest = jax.ops.segment_sum(grad_pre_edge, edge_dst, row_count)
    grad_extended = jax.ops.segment_sum(
        jnp.concatenate([numer_edge * gating, grad_pre_edge], 1),
        edge_src,
        row_count + halo_send.shape[0],
    )
    returned = return_sources(grad_extended[row_count:])
    grad_source = grad_extended[:row_count].at[halo_send].add(returned)
    proj_grad = jnp.concatenate(
        [grad_message, grad_source[:, :model_width], grad_dest, grad_source[:, model_width:]], 1
    ).astype(jnp.bfloat16)
    grad_w_proj = outer_product(hidden_low, proj_grad)
    grad_hidden = (
        grad_mixed
        + grad_two
        + times_transposed(proj_grad, w_proj)
        + times_transposed(qkv_grad, w_qkv)
    )
    weight_grads = (grad_w_proj, grad_w_edge, grad_w_qkv, grad_w_out, grad_w_up, grad_w_down)
    return (
        grad_hidden,
        weight_grads,
        jnp.stack([gain_one, gain_two, gain_three]),
        jnp.stack([shift_one, shift_two, shift_three]),
    )


def per_device(
    node_input,
    edge_feat,
    graph_ids,
    edge_src,
    edge_dst,
    halo_send,
    w_proj,
    w_edge,
    w_qkv,
    w_out,
    w_up,
    w_down,
    norm_gain,
    norm_shift,
    cotangent,
):
    group_graphs = lax.all_gather(graph_ids, "nodes", axis=0, tiled=True)
    node_total = node_input.shape[0] * lax.axis_size("nodes") * lax.axis_size("rep")
    layer_count = w_proj.shape[0]
    layer_params = [
        (
            w_proj[layer_index],
            w_edge[layer_index],
            w_qkv[layer_index],
            w_out[layer_index],
            w_up[layer_index],
            w_down[layer_index],
            norm_gain[layer_index],
            norm_shift[layer_index],
        )
        for layer_index in range(layer_count)
    ]
    hidden = node_input.astype(jnp.float32)
    saved_all = []
    for layer_index in range(layer_count):
        hidden, saved = layer_forward(
            hidden,
            layer_params[layer_index],
            edge_feat,
            edge_src,
            edge_dst,
            halo_send,
            graph_ids,
            group_graphs,
            node_total,
        )
        saved_all.append(saved)
    grad_hidden = cotangent.astype(jnp.float32)
    weight_parts = [None] * layer_count
    gain_parts = [None] * layer_count
    shift_parts = [None] * layer_count
    for layer_index in range(layer_count - 1, -1, -1):
        (
            grad_hidden,
            weight_parts[layer_index],
            gain_parts[layer_index],
            shift_parts[layer_index],
        ) = layer_backward(
            grad_hidden,
            layer_params[layer_index],
            saved_all[layer_index],
            edge_feat,
            edge_src,
            edge_dst,
            halo_send,
            graph_ids,
            group_graphs,
            node_total,
        )
    proj_local = jnp.stack([weight_parts[layer_index][0] for layer_index in range(layer_count)])
    edge_local = jnp.stack([weight_parts[layer_index][1] for layer_index in range(layer_count)])
    qkv_local = jnp.stack([weight_parts[layer_index][2] for layer_index in range(layer_count)])
    out_local = jnp.stack([weight_parts[layer_index][3] for layer_index in range(layer_count)])
    up_local = jnp.stack([weight_parts[layer_index][4] for layer_index in range(layer_count)])
    down_local = jnp.stack([weight_parts[layer_index][5] for layer_index in range(layer_count)])
    grad_proj, grad_edge, grad_qkv, grad_out, grad_up, grad_down = lax.psum(
        (proj_local, edge_local, qkv_local, out_local, up_local, down_local), ("nodes", "rep")
    )
    return (
        hidden,
        grad_hidden,
        grad_proj,
        grad_edge,
        grad_qkv,
        grad_out,
        grad_up,
        grad_down,
        jnp.stack(gain_parts),
        jnp.stack(shift_parts),
    )


def solution(mesh):
    in_specs = (
        P(("rep", "nodes"), None),
        P(("rep", "nodes"), None),
        P(("rep", "nodes")),
        P(("rep", "nodes")),
        P(("rep", "nodes")),
        P(("rep", "nodes")),
        P(),
        P(),
        P(),
        P(),
        P(),
        P(),
        P(),
        P(),
        P(("rep", "nodes"), None),
    )
    out_specs = (
        P(("rep", "nodes"), None),
        P(("rep", "nodes"), None),
        P(),
        P(),
        P(),
        P(),
        P(),
        P(),
        P(),
        P(),
    )
    N, M = mesh.shape["nodes"], mesh.shape["rep"]
    fused = N in (4, 8) and M % 2 == 0 and 512 % (16 * N * M) == 0
    return jax.shard_map(
        functools.partial(fused_device, N, M) if fused else per_device,
        mesh=mesh, in_specs=in_specs, out_specs=out_specs, check_vma=False,
    )
```

```python
import functools
import math

import jax
import jax.numpy as jnp
from jax import lax
from jax.experimental import pallas as pl
from jax.experimental.pallas import tpu as pltpu
from jax.sharding import PartitionSpec as P

HEADS = 8
HEAD_DIM = 32
NEG = -1e30
NORM_EPS = 1e-05
GATE_EPS = 1e-06
F32, BF16, I32 = jnp.float32, jnp.bfloat16, jnp.int32
MESH = pl.DeviceIdType.MESH
SYNCS = 12
STRIP = 32
GROUPS = (
    ("early", 1, 0, 2560, ("core", "y", "nodes")),
    ("conv", 1, 0, 2560, ("core", "y", "nodes")),
    ("qkv", 1, 0, 1536, ("core", "y", "nodes")),
    ("early", 0, 0, 2560, ("core", "y", "nodes")),
    ("conv", 0, 0, 2560, ("core", "y", "nodes")),
    ("qkv", 0, 0, 1024, ("rep", "nodes")),
    ("qkv", 0, 1024, 512, ("nodes", "rep")),
)


def dot(left, right):
    return lax.dot_general(
        left, right, (((1,), (0,)), ((), ())), preferred_element_type=F32
    )


def dot_nt(left, right):
    return lax.dot_general(
        left, right, (((1,), (1,)), ((), ())), preferred_element_type=F32
    )


def dot_tn(left, right):
    return lax.dot_general(
        left, right, (((0,), (0,)), ((), ())), preferred_element_type=F32
    )


def split(value):
    high = value.astype(BF16)
    return high, (value - high.astype(F32)).astype(BF16)


def sigmoid(value):
    return jax.nn.sigmoid(value)


def silu_slope(value):
    logistic = sigmoid(value)
    return logistic * (1.0 + value * (1.0 - logistic))


def col_sum(value):
    return jnp.sum(value, axis=0, keepdims=True)


def pack(first, second):
    return jnp.concatenate([first[:, :128], first[:, 128:], second[:, :128], second[:, 128:]], 0)


def unpack(tile):
    return [jnp.concatenate([tile[i : i + 1], tile[i + 1 : i + 2]], 1) for i in (0, 2)]


def combine_moments(tiles, count):
    mean = jnp.mean(tiles[:, 0:2], 0)
    off = tiles[:, 0:2] - mean
    return jnp.concatenate([mean, jnp.sum(tiles[:, 2:4] + count * off * off, 0)], 0)


class Refs:
    pass


def axis_sizes(N, M):
    return dict(core=2, y=M // 2, x=2, z=N // 2, rep=M, nodes=N)


def scratch_list(N, M, L, R, E):
    NZ, NB, G = N // 2, N // 4, N * R
    D, FF, W, HH = 256, 512, 4 * R, HEADS // 2 * R
    dma = lambda *shape: pltpu.SemaphoreType.DMA(shape)
    vm = lambda dtype, *shape: pltpu.VMEM(shape, dtype)
    names = dict(
        gb=vm(BF16, L, N, R, D),
        xs=vm(BF16, L, N, R, D),
        meta=vm(I32, N, 8, 256),
        cot=vm(BF16, R, D),
        wp=vm(BF16, L, D, 4 * D),
        we=vm(BF16, L, D, D),
        wqkv=vm(BF16, L, D, 3 * D),
        wo=vm(BF16, L, D, D),
        wu=vm(BF16, L, D, FF),
        wd=vm(BF16, L, FF, D),
        st1=vm(F32, SYNCS, M * N, 4, 128),
        gain=vm(F32, L, 8, D),
        shift=vm(F32, L, 8, D),
        ggain=vm(F32, L, 8, D),
        gshift=vm(F32, L, 8, D),
        iv=vm(F32, L, 8, D),
        moff=vm(F32, N, 8, D),
        move=vm(F32, 8, D),
        le=vm(BF16, E, 1024),
        re=vm(BF16, 1024, D),
        TT=vm(BF16, R, 2 * E),
        ST=vm(BF16, 256, E),
        efT=vm(BF16, D, E),
        HS=vm(BF16, 64, R),
        hx=vm(BF16, L, 64, D),
        A=vm(BF16, R, 64),
        bias=vm(F32, R, G),
        xf=vm(F32, L + 1, R, D),
        xe=vm(BF16, L, 256, D),
        xeT=vm(BF16, D, 256),
        gate=vm(F32, L, E, D),
        bs=vm(BF16, L, E, D),
        num=vm(F32, L, R, D),
        den=vm(F32, L, R, D),
        z0=vm(F32, L, R, D),
        z1=vm(F32, L, R, D),
        z2=vm(F32, L, R, D),
        wkvT=vm(BF16, L, 2 * D, D),
        kvT=vm(BF16, L, 2 * D, G),
        odT=vm(F32, NB, D, R),
        ldT=vm(F32, NB, D, R),
        md=vm(F32, NB, R, D),
        rb=vm(F32, L, NB, R, D),
        pst=vm(BF16, L, HEADS * R, G),
        oraw=vm(F32, L, R, D),
        ob=vm(BF16, L, R, D),
        mb=vm(BF16, L, R, D),
        u=vm(F32, L, R, FF),
        g=vm(BF16, L, R, FF),
        dy=vm(F32, R, D),
        dmix=vm(F32, R, D),
        gy0=vm(F32, R, D),
        local=vm(F32, R, D),
        dxo=vm(F32, R, D),
        dob=vm(F32, R, D),
        dqT=vm(F32, D, R),
        qm=vm(BF16, L, 2, HH, 128),
        q=vm(BF16, L, R, D),
        qT=vm(BF16, D, R),
        dosT=vm(BF16, 128, R),
        dom=vm(BF16, HH, 256),
        sc=vm(F32, 2, max(2 * R, E), W),
        tp=vm(F32, HEADS // 2, R, 128),
        dss=vm(BF16, HH, W),
        dkv=vm(BF16, 2 * D, W),
        gkv=vm(F32, 2 * D, D),
        gg=vm(BF16, 2 * E, 2 * D),
        dn=vm(BF16, 512, 2 * D),
        dproj=vm(BF16, 256, 4 * D),
        dxs=vm(BF16, L, NZ, 2, R, D),
        rs1=vm(BF16, L, NZ, R, D),
        cs=vm(BF16, L, NZ, R, D),
        rs2=vm(BF16, L, NZ, R, D),
        ro=vm(BF16, L, 3, R, D),
        hs=vm(BF16, L, 2, 32, D),
        hr=vm(BF16, L, 2, 32, D),
    )
    names.update(
        gs_early=vm(BF16, L, 2560, 128),
        gs_conv=vm(BF16, L, 2560, 128),
        gs_qkv=vm(BF16, L, 1536, 128),
    )
    sizes = axis_sizes(N, M)
    for g, (_, _, _, rows, stages) in enumerate(GROUPS):
        names[f"go{g}"] = vm(BF16, rows, 128)
        left = rows
        for k, axis in enumerate(stages):
            left //= sizes[axis]
            names[f"ga{g}_{k}"] = vm(BF16, sizes[axis] - 1, left, 128)
            if k < len(stages) - 1:
                names[f"gh{g}_{k}"] = vm(BF16, left, 128)
    names.update(
        ar_s=dma(len(GROUPS)),
        ar_r=dma(sum(2 * len(stages) for *_, stages in GROUPS)),
        ar_l=dma(len(GROUPS)),
        load=dma(9),
        store=dma(2),
        meta_s=dma(1),
        meta_r=dma(1),
        st_s=dma(1),
        st_r=dma(SYNCS),
        ag_s=dma(1),
        agn_r=dma(L),
        agc_r=dma(L, NZ),
        agp_r=dma(L),
        rs_s=dma(1),
        rsp_r=dma(L, NB, 2),
        ro_r=dma(L),
        rsc_r=dma(L),
        hx_s=dma(1),
        hx_r=dma(L),
        hal_s=dma(1),
        hal_r=dma(L),
    )
    return names


IN_NAMES = (
    "x_in", "ids", "edge_src", "edge_dst", "halo", "ef_h", "wp_h", "we_h", "wqkv_h", "wo_h", "wu_h", "wd_h",
    "gain_in", "shift_in", "cot_h",
)
OUT_NAMES = ("out_act", "grad_in", *(f"gout{g}" for g in range(len(GROUPS))), "ggain_out", "gshift_out")


def kernel(N, M, L, names, *args):
    r_ = Refs()
    for name, ref in zip(IN_NAMES + OUT_NAMES + tuple(names), args, strict=True):
        setattr(r_, name, ref)
    R, D = r_.x_in.shape
    E = r_.ef_h.shape[0]
    NZ, NB, G, W = N // 2, N // 4, N * R, 4 * R
    HK = HEADS // 2
    total = float(N * M * R)
    scale = HEAD_DIM ** -0.5
    me = lax.axis_index("nodes")
    rep = lax.axis_index("rep")
    z = me // 2
    par = me % 2
    partner = 2 * z + (1 - par)
    prev = (me + N - 1) % N
    nxt = (me + 1) % N
    zh, zl = z // 2, z % 2
    z_to = lambda t: 2 * ((zh + t // 2) % NB) + (zl + t % 2) % 2
    z_from = lambda t: 2 * ((zh + NB - t // 2) % NB) + (zl + t % 2) % 2

    def remote(src, dst, s_sem, r_sem, **where):
        return pltpu.make_async_remote_copy(
            src_ref=src, dst_ref=dst, send_sem=s_sem, recv_sem=r_sem,
            device_id=where, device_id_type=MESH,
        )

    def send(src, dst, s_sem, r_sem, **where):
        remote(src, dst, s_sem, r_sem, **where).start()

    def send_rows(src, dst, rows, s_sem, r_sem, **where):
        pieces = next(p for p in range(1, rows) if rows % (16 * p) == 0 and rows // p <= 128)
        for at in range(0, rows, rows // pieces):
            cut = pl.ds(at, rows // pieces)
            send(src.at[cut], dst.at[cut], s_sem, r_sem, **where)

    def arrive(dst, r_sem):
        remote(dst, dst, r_sem, r_sem, nodes=partner).wait_recv()

    def sent(src, s_sem):
        remote(src, src, s_sem, s_sem, nodes=partner).wait_send()

    def when(condition, *acts):
        if condition:
            for act in acts:
                act()

    loads = [pltpu.make_async_copy(r_.ef_h, r_.le.at[:, D : 2 * D], r_.load.at[0])] + [
        pltpu.make_async_copy(getattr(r_, f"{name}_h"), getattr(r_, name), r_.load.at[1 + i])
        for i, name in enumerate(("we", "wqkv", "wp", "wo", "wu", "wd", "cot"))
    ]
    own_rows = pltpu.make_async_copy(r_.x_in, r_.gb.at[0, me], r_.load.at[8])
    own_rows.start()
    for load in loads:
        load.start()

    barrier = pltpu.get_barrier_semaphore()
    for dr in range(M):
        for d in range(N):
            if dr + d > 0:
                pl.semaphore_signal(barrier, inc=1, device_id={"rep": (rep + dr) % M, "nodes": (me + d) % N},
                                    device_id_type=MESH)

    def gather_start(l):
        mine = r_.gb.at[l, me]
        for t in range(2, NZ):
            send_rows(mine, mine, R, r_.ag_s.at[0], r_.agc_r.at[l, t], nodes=2 * z_to(t) + par)
        send_rows(mine, mine, R, r_.ag_s.at[0], r_.agn_r.at[l], nodes=partner)
        send_rows(mine, mine, R, r_.ag_s.at[0], r_.agn_r.at[l], nodes=2 * z_to(1) + par)
        send_rows(mine, mine, R, r_.ag_s.at[0], r_.agn_r.at[l], nodes=2 * z_to(1) + 1 - par)

    def gather_pass(l, t):
        piece = r_.gb.at[l, 2 * z_from(t) + par]
        arrive(piece, r_.agc_r.at[l, t])
        send_rows(piece, piece, R, r_.ag_s.at[0], r_.agp_r.at[l], nodes=partner)

    def gather_near(l):
        arrive(r_.gb.at[l, 0:3], r_.agn_r.at[l])

    def gather_far(l):
        arrive(r_.gb.at[l, 0 : NZ - 2], r_.agp_r.at[l])

    def sync_start(k, first, second):
        mine = rep * N + me
        r_.st1[k, mine] = pack(first, second)
        for dr in range(M):
            for d in range(N):
                if dr + d > 0:
                    send(r_.st1.at[k, mine], r_.st1.at[k, mine], r_.st_s.at[0], r_.st_r.at[k],
                         rep=(rep + dr) % M, nodes=(me + d) % N)

    def sync_wait(k):
        arrive(r_.st1.at[k, 0 : M * N - 1], r_.st_r.at[k])

    def sync_moments(k):
        sync_wait(k)
        return unpack(combine_moments(r_.st1[k], float(R)))

    def sync_sums(k):
        sync_wait(k)
        return unpack(jnp.sum(r_.st1[k], 0))

    sizes = axis_sizes(N, M)
    core, row = rep % 2, rep // 2
    places = dict(
        core=(core, lambda t: dict(rep=2 * row + t)),
        y=(row, lambda t: dict(rep=2 * t + core)),
        x=(par, lambda t: dict(nodes=2 * z + t)),
        z=(z, lambda t: dict(nodes=2 * t + par)),
        rep=(rep, lambda t: dict(rep=t)),
        nodes=(me, lambda t: dict(nodes=t)),
    )

    def reduce_step(g, step):
        name, layer, first, rows, stages = GROUPS[g]
        K = len(stages)
        base = sum(2 * len(before) for *_, before in GROUPS[:g])
        gs, out = getattr(r_, f"gs_{name}").at[layer, first : first + rows], getattr(r_, f"go{g}")
        count, offset = [rows], [0]
        for axis in stages:
            count.append(count[-1] // sizes[axis])
            offset.append(offset[-1] + places[axis][0] * count[-1])
        take = lambda start, size: pl.ds(pl.multiple_of(start, 16), size)
        if 1 <= step <= K:
            k = step - 1
            got = getattr(r_, f"ga{g}_{k}")
            arrive(got, r_.ar_r.at[base + k])
            held = gs if k == 0 else getattr(r_, f"gh{g}_{k - 1}")
            index = places[stages[k]][0]
            acc = held[take(index * count[k + 1], count[k + 1])].astype(F32)
            for slot in range(sizes[stages[k]] - 1):
                acc = acc + got[slot].astype(F32)
            if step < K:
                getattr(r_, f"gh{g}_{k}")[...] = acc.astype(BF16)
            else:
                out[take(offset[K], count[K])] = acc.astype(BF16)
        elif step > K:
            k = 2 * K - step
            arrive(out.at[0 : (sizes[stages[k]] - 1) * count[k + 1]], r_.ar_r.at[base + step - 1])
        if step < K:
            held = gs if step == 0 else getattr(r_, f"gh{g}_{step - 1}")
            index, device = places[stages[step]]
            size = sizes[stages[step]]
            for d in range(1, size):
                to = (index + d) % size
                send_rows(held.at[take(to * count[step + 1], count[step + 1])], getattr(r_, f"ga{g}_{step}").at[d - 1],
                     count[step + 1], r_.ar_s.at[g], r_.ar_r.at[base + step], **device(to))
        elif step < 2 * K:
            k = 2 * K - 1 - step
            index, device = places[stages[k]]
            size = sizes[stages[k]]
            here = out.at[take(offset[k + 1], count[k + 1])]
            for d in range(1, size):
                send_rows(here, here, count[k + 1], r_.ar_s.at[g], r_.ar_r.at[base + step],
                          **device((index + d) % size))
        else:
            pltpu.make_async_copy(out, getattr(r_, f"gout{g}"), r_.ar_l.at[g]).start()

    def reduce_drain(g):
        name, _, _, rows, _ = GROUPS[g]
        sent(getattr(r_, f"gs_{name}").at[:, 0 : rows - rows // (M * N)], r_.ar_s.at[g])
        pltpu.make_async_copy(getattr(r_, f"go{g}"), getattr(r_, f"gout{g}"), r_.ar_l.at[g]).wait()

    def put(buf, l, at, value):
        rows = value.shape[0]
        for c in range(value.shape[1] // 128):
            buf[l, at : at + rows] = value[:, 128 * c : 128 * (c + 1)].astype(BF16)
            at += rows
        return at

    lane_head = lax.broadcasted_iota(I32, (R, 128), 1) // HEAD_DIM

    def by_head(parts):
        out = parts[0]
        for k in range(1, HK):
            out = jnp.where(lane_head == k, parts[k], out)
        return out

    r_.meta[me] = jnp.full((8, 256), -1, I32)
    r_.meta[me, 0:1, 0:R] = r_.ids[...].reshape(1, R)
    r_.meta[me, 1:2, 0:48] = r_.halo[...].reshape(1, 48)
    src_row = r_.edge_src[...].reshape(1, E)
    src_row = jnp.where(src_row < R + 24, src_row, src_row + 8)
    dst_row = r_.edge_dst[...].reshape(1, E)
    src_col = jnp.broadcast_to(src_row, (128, E)).T[:, 0:1]
    dst_col = jnp.broadcast_to(dst_row, (128, E)).T[:, 0:1]
    as_mask = lambda cond: cond.astype(F32).astype(BF16)
    r_.le[:, 0:256] = as_mask(src_col == lax.broadcasted_iota(I32, (E, 256), 1))
    target = as_mask(dst_col == lax.broadcasted_iota(I32, (E, 256), 1))
    r_.le[:, 512:768] = target
    r_.le[:, 768:1024] = target
    target = as_mask(dst_row == lax.broadcasted_iota(I32, (R, E), 0))
    r_.TT[:, 0:E] = target
    r_.TT[:, E:] = target
    r_.ST[...] = as_mask(src_row == lax.broadcasted_iota(I32, (256, E), 0))
    r_.dn[R:256] = jnp.zeros((256 - R, 2 * D), BF16)
    r_.dn[256 + R : 512] = jnp.zeros((256 - R, 2 * D), BF16)
    r_.dproj[R:256, 0:D] = jnp.zeros((256 - R, D), BF16)
    r_.dproj[R:256, 2 * D : 3 * D] = jnp.zeros((256 - R, D), BF16)
    halo_col = jnp.broadcast_to(r_.meta[me][1:2, 0:128], (128, 128)).T
    hot = (halo_col[0:48, 0:1] == lax.broadcasted_iota(I32, (48, R), 1)).astype(F32)
    pad = jnp.zeros((8, R), F32)
    r_.HS[...] = jnp.concatenate([hot[0:24], pad, hot[24:48], pad], 0).astype(BF16)
    r_.A[...] = as_mask(r_.meta[me][1:2, 0:64] == lax.broadcasted_iota(I32, (R, 64), 0))
    own_rows.wait()
    pl.semaphore_wait(barrier, M * N - 1)
    gather_start(0)
    for d in range(1, N):
        send(r_.meta.at[me], r_.meta.at[me], r_.meta_s.at[0], r_.meta_r.at[0], nodes=(me + d) % N)
    loads[0].wait()
    r_.efT[...] = r_.le[:, D : 2 * D].T
    for l in range(L):
        for k in range(3):
            r_.gain[l, k : k + 1] = r_.gain_in[k, l : l + 1]
            r_.shift[l, k : k + 1] = r_.shift_in[k, l : l + 1]
    r_.xf[0] = r_.gb[0, me].astype(F32)
    r_.moff[...] = jnp.zeros((N, 8, D), F32)
    r_.move[0:1] = jnp.ones((1, D), F32)
    r_.move[1:2] = jnp.zeros((1, D), F32)
    for load in loads[1:]:
        load.wait()
    for l in range(L):
        r_.wkvT[l] = r_.wqkv[l, :, D:].T

    arrive(r_.meta.at[0 : N - 1], r_.meta_r.at[0])
    id_col = jnp.broadcast_to(r_.meta[me][0:1, 0:R], (128, R)).T[:, 0:1]
    id_row = jnp.concatenate(
        [r_.meta[4 * ((zh + NB - j // 4) % NB) + j % 4][0:1, 0:R] for j in range(N)], 1
    )
    r_.bias[...] = jnp.where(id_col == id_row, 0.0, NEG)

    factor_exp = scale * math.log2(math.e)

    def prepare_queries(l):
        q = dot(r_.xs[l, me], r_.wqkv[l, :, :D]).astype(BF16)
        r_.q[l] = q
        q = q.astype(F32)
        for hf in range(2):
            for k in range(HK):
                part = jnp.where(lane_head == k, q[:, 128 * hf : 128 * (hf + 1)], 0.0)
                r_.qm[l, hf, k * R : (k + 1) * R] = part.astype(BF16)

    def head_dims(hf, k, base=0):
        first = base + hf * 128 + k * HEAD_DIM
        return slice(first, first + HEAD_DIM)

    def head_rows(hf, k, count=1):
        return slice((hf * HK + k) * R, (hf * HK + k + count) * R)

    def lane_half(hf):
        return slice(hf * 128, (hf + 1) * 128)

    def half_of(i):
        return (zh + NB - i) % NB, slice(i * W, (i + 1) * W)

    def attention_keys(l, i):
        half, rows = half_of(i)
        x = r_.xs[l, pl.ds(4 * half, 4)].reshape(W, D)
        r_.kvT[l, :, rows] = dot_nt(r_.wkvT[l], x).astype(BF16)

    def attention_heads(l, i, hfs):
        _, rows = half_of(i)
        for hf in hfs:
            lanes = lane_half(hf)
            ones = jnp.ones((HEAD_DIM, W), BF16)
            for c in range(HK // 2):
                r_.sc[c % 2, 0 : 2 * R] = dot(r_.qm[l, hf, 2 * c * R : 2 * (c + 1) * R], r_.kvT[l, lanes, rows])
                for k in range(2):
                    for at in range(0, R, STRIP):
                        s = r_.sc[c % 2, k * R + at : k * R + at + STRIP] + r_.bias[at : at + STRIP, rows]
                        top = jnp.max(s, 1, keepdims=True)
                        e = jnp.exp2((s - top) * factor_exp)
                        r_.tp[2 * c + k, at : at + STRIP] = jnp.broadcast_to(top, (STRIP, 128))
                        first = (hf * HK + 2 * c + k) * R + at
                        r_.pst[l, first : first + STRIP, rows] = e.astype(BF16)
                for k in range(2):
                    h = 2 * c + k
                    left = jnp.concatenate([r_.kvT[l, head_dims(hf, h, D), rows], ones], 0)
                    o = dot_nt(left, r_.pst[l, head_rows(hf, h), rows])
                    r_.odT[i, head_dims(hf, h)] = o[0:HEAD_DIM]
                    r_.ldT[i, head_dims(hf, h)] = o[HEAD_DIM:]
            r_.md[i, :, lanes] = by_head([r_.tp[k] for k in range(HK)])

    def attention_end(l):
        tops = [r_.md[i].T for i in range(NB)]
        top = tops[0]
        for i in range(1, NB):
            top = jnp.maximum(top, tops[i])
        factors = [jnp.exp2((tops[i] - top) * factor_exp) for i in range(NB)]
        inv = 1.0 / sum(factors[i] * r_.ldT[i] for i in range(NB))
        o = jnp.zeros((D, R), F32)
        for i in range(NB):
            r_.rb[l, i] = (factors[i] * inv).T
            o = o + factors[i] * inv * r_.odT[i]
        o = o.T
        r_.oraw[l] = o
        ob = o.astype(BF16)
        r_.ob[l] = ob
        t1 = r_.xf[l] + dot(ob, r_.wo[l])
        r_.z1[l] = t1
        mean1 = col_sum(t1) / R
        return mean1, col_sum((t1 - mean1) * (t1 - mean1))

    def convolution(l):
        xs = r_.xs
        xb = xs[l, me]
        r_.xe[l, 0:R] = xb
        arrive(r_.xe.at[l, R : R + 64], r_.hx_r.at[l])
        xe = r_.xe[l]
        made = dot(xe, r_.wp[l])
        pd_high, pd_low = split(made[:, 2 * D : 3 * D])
        r_.re[0:256] = made[:, 3 * D :].astype(BF16)
        r_.re[256:512] = r_.we[l]
        r_.re[512:768] = pd_high
        r_.re[768:1024] = pd_low
        r_.gate[l] = dot(r_.le[...], r_.re[...])
        r_.bs[l] = dot(r_.le[:, 0:256], made[:, D : 2 * D].astype(BF16)).astype(BF16)
        for at in range(0, E, 64):
            here = slice(at, at + 64)
            gate = sigmoid(r_.gate[l, here])
            r_.gate[l, here] = gate
            high, low = split(jnp.concatenate([gate * r_.bs[l, here].astype(F32), gate], 1))
            r_.gg[here] = high
            r_.gg[E + at : E + at + 64] = low
        num_den = dot(r_.TT[...], r_.gg[...])
        pa, num, den = made[0:R, 0:D], num_den[:, 0:D], num_den[:, D:]
        r_.num[l] = num
        r_.den[l] = den
        msg = pa + num / (den + GATE_EPS)
        r_.z0[l] = msg
        mean0 = col_sum(msg) / R
        return mean0, col_sum((msg - mean0) * (msg - mean0))

    def forward(l):
        def ready(js):
            for j in js:
                moved = (r_.gb[l, j].astype(F32) + r_.moff[j, 0:1]) * r_.move[0:1] + r_.move[1:2]
                r_.xs[l, j] = moved.astype(BF16)

        r_.xs[l, me] = r_.xf[l].astype(BF16)
        r_.hx[l] = dot(r_.HS[...], r_.xs[l, me]).astype(BF16)
        send(r_.hx.at[l, 0:32], r_.xe.at[l, R + 32 : R + 64], r_.hx_s.at[0], r_.hx_r.at[l], nodes=prev)
        send(r_.hx.at[l, 32:64], r_.xe.at[l, R : R + 32], r_.hx_s.at[0], r_.hx_r.at[l], nodes=nxt)
        prepare_queries(l)
        for t in range(2, NZ):
            gather_pass(l, t)
        mean0, sq0 = convolution(l)
        sync_start(3 * l, mean0, sq0)
        gather_near(l)
        ready([partner, 2 * z_from(1) + par, 2 * z_from(1) + 1 - par])

        attention_keys(l, 0)
        attention_heads(l, 0, (0, 1))
        gather_far(l)
        ready([2 * z_from(t) + p for t in range(2, NZ) for p in range(2)])
        for i in range(1, NB):
            attention_keys(l, i)
            attention_heads(l, i, (0, 1))
        mean1, sq1 = attention_end(l)
        sync_start(3 * l + 1, mean1, sq1)
        mean0, sq0 = sync_moments(3 * l)
        inv0 = lax.rsqrt(sq0 / total + NORM_EPS)
        r_.iv[l, 0:1] = inv0
        z0 = (r_.z0[l] - mean0) * inv0
        r_.z0[l] = z0
        n0 = z0 * r_.gain[l, 0:1] + r_.shift[l, 0:1]
        r_.local[...] = r_.xf[l] + n0 * sigmoid(n0)
        mean1, sq1 = sync_moments(3 * l + 1)
        inv1 = lax.rsqrt(sq1 / total + NORM_EPS)
        r_.iv[l, 1:2] = inv1
        z1 = (r_.z1[l] - mean1) * inv1
        r_.z1[l] = z1
        mix = r_.local[...] + z1 * r_.gain[l, 1:2] + r_.shift[l, 1:2]
        mb = mix.astype(BF16)
        r_.mb[l] = mb
        u = dot(mb, r_.wu[l])
        r_.u[l] = u
        g = (u * sigmoid(u)).astype(BF16)
        r_.g[l] = g
        y = mix + dot(g, r_.wd[l])
        r_.z2[l] = y
        mean = col_sum(y) / R
        cent = y - mean
        k = 3 * l + 2
        sync_start(k, mean, col_sum(cent * cent))

        if l < L - 1:
            r_.gb[l + 1, me] = cent.astype(BF16)
            gather_start(l + 1)

        if l == L - 1:
            dy = r_.cot[...].astype(F32)
            sync_start(3 * L, col_sum(dy), col_sum(dy * cent))

        tot_mean, tot_sq = sync_moments(k)
        inv2 = lax.rsqrt(tot_sq / total + NORM_EPS)
        r_.iv[l, 2:3] = inv2
        z2 = (r_.z2[l] - tot_mean) * inv2
        r_.z2[l] = z2
        gain, shift = r_.gain[l, 2:3], r_.shift[l, 2:3]
        r_.xf[l + 1] = z2 * gain + shift

        if l == L - 1:
            sync_wait(3 * L)
            sums, means = r_.st1[3 * L], r_.st1[k][:, 0:2]
            mean = jnp.mean(means, 0)
            dy_sum = jnp.sum(sums[:, 0:2], 0)
            dy_cent = jnp.sum(sums[:, 2:4] + (means - mean) * sums[:, 0:2], 0)
            dy_sum, dy_cent = unpack(jnp.concatenate([dy_sum, dy_cent], 0))
            r_.gshift[l, 2:3] = dy_sum
            r_.ggain[l, 2:3] = dy_cent * inv2

        for j in range(N):
            tile = r_.st1[k, rep * N + j]
            r_.moff[j, 0:1] = jnp.concatenate([tile[0:1], tile[1:2]], 1) - tot_mean
        r_.move[0:1] = inv2 * gain
        r_.move[1:2] = shift

    for l in range(L):
        forward(l)
    act_copy = pltpu.make_async_copy(r_.xf.at[L], r_.out_act, r_.store.at[0])
    act_copy.start()

    def back_feed_forward(l, k):
        s2, g2 = r_.gshift[l, 2:3], r_.ggain[l, 2:3]
        d3 = r_.gain[l, 2:3] * r_.iv[l, 2:3] * (r_.dy[...] - s2 / total - r_.z2[l] * (g2 / total))
        db = d3.astype(BF16)
        dub = (dot_nt(db, r_.wd[l]) * silu_slope(r_.u[l])).astype(BF16)
        dmix = d3 + dot_nt(dub, r_.wu[l])
        r_.dmix[...] = dmix
        n0 = r_.z0[l] * r_.gain[l, 0:1] + r_.shift[l, 0:1]
        gy0 = dmix * silu_slope(n0)
        sync_start(k, col_sum(dmix), col_sum(dmix * r_.z1[l]))
        sync_start(k + 1, col_sum(gy0), col_sum(gy0 * r_.z0[l]))
        r_.gy0[...] = gy0
        at = put(r_.gs_early, l, 512, dot_tn(r_.mb[l], dub))
        put(r_.gs_early, l, at, dot_tn(r_.g[l], db))
        r_.xeT[...] = r_.xe[l].T
        r_.qT[...] = r_.q[l].T

    def back_norms(l, k):
        s1, g1 = sync_sums(k)
        r_.gshift[l, 1:2] = s1
        r_.ggain[l, 1:2] = g1
        dmix = r_.dmix[...]
        d2 = r_.gain[l, 1:2] * r_.iv[l, 1:2] * (dmix - s1 / total - r_.z1[l] * (g1 / total))
        dab = d2.astype(BF16)
        r_.dxo[...] = dmix + d2
        r_.dob[...] = dot_nt(dab, r_.wo[l]).astype(BF16).astype(F32)
        put(r_.gs_early, l, 0, dot_tn(r_.ob[l], dab))
        r_.gkv[...] = jnp.zeros((2 * D, D), F32)
        r_.dqT[...] = jnp.zeros((D, R), F32)

    def back_half(i):
        t1 = (i + 1) % NB
        half = (zh + t1) % NB
        place = (NB - t1) % NB
        return place, half, slice(place * W, (place + 1) * W)

    def back_heads(l, i, hf):
        place, half, rows = back_half(i)
        if True:
            lanes = lane_half(hf)
            dos = r_.dob[:, lanes] * r_.rb[l, place, :, lanes]
            prod = dos * r_.oraw[l, :, lanes]
            for k in range(HK):
                r_.dom[k * R : (k + 1) * R, 0:128] = jnp.where(lane_head == k, dos, 0.0).astype(BF16)
                r_.dom[k * R : (k + 1) * R, 128:256] = jnp.where(lane_head == k, -prod, 0.0).astype(BF16)
            r_.dosT[...] = dos.T.astype(BF16)
            values = slice(D + hf * 128, D + (hf + 1) * 128)
            right = jnp.concatenate([r_.kvT[l, values, rows], jnp.ones((128, W), BF16)], 0)
            for c in range(HK // 2):
                both = slice(2 * c * R, 2 * (c + 1) * R)
                r_.sc[c % 2, 0 : 2 * R] = dot(r_.dom[both], right)
                for k in range(2):
                    for at in range(0, R, STRIP):
                        first = (hf * HK + 2 * c + k) * R + at
                        e = r_.pst[l, first : first + STRIP, rows].astype(F32)
                        ds = e * r_.sc[c % 2, k * R + at : k * R + at + STRIP]
                        r_.dss[(2 * c + k) * R + at : (2 * c + k) * R + at + STRIP] = ds.astype(BF16)
                for k in range(2):
                    h = 2 * c + k
                    mine, dims = slice(h * R, (h + 1) * R), head_dims(hf, h)
                    r_.dqT[dims] += dot_nt(r_.kvT[l, dims, rows], r_.dss[mine])
                    r_.dkv[dims] = (dot(r_.qT[dims], r_.dss[mine]) * scale).astype(BF16)
                    dv = dot(r_.dosT[h * HEAD_DIM : (h + 1) * HEAD_DIM], r_.pst[l, head_rows(hf, h), rows])
                    r_.dkv[head_dims(hf, h, D)] = dv.astype(BF16)

    def back_rows(l, i):
        _, half, _ = back_half(i)
        dx = dot(r_.wqkv[l, :, D:], r_.dkv[...]).T
        r_.dxs[l, pl.ds(2 * half, 2)] = dx.astype(BF16).reshape(2, 2, R, D)

        if i < NB - 1:
            for t in (2 * (i + 1), 2 * (i + 1) + 1):
                zb = z_to(t)
                send_rows(r_.dxs.at[l, zb, 1 - par], r_.rs1.at[l, zb], R,
                          r_.rs_s.at[0], r_.rsp_r.at[l, i, t % 2], nodes=partner)

        else:
            near = z_to(1)
            send_rows(r_.dxs.at[l, z, 1 - par], r_.ro.at[l, 0], R, r_.rs_s.at[0], r_.ro_r.at[l], nodes=partner)
            send_rows(r_.dxs.at[l, near, par], r_.ro.at[l, 1], R, r_.rs_s.at[0], r_.ro_r.at[l], nodes=2 * near + par)
            send_rows(r_.dxs.at[l, near, 1 - par], r_.ro.at[l, 2], R, r_.rs_s.at[0], r_.ro_r.at[l],
                 nodes=2 * near + 1 - par)

        r_.gkv[...] += dot(r_.dkv[...], r_.xs[l, pl.ds(4 * half, 4)].reshape(W, D))

    def pass_on(l, i, t):
        zb = z_to(t)
        arrive(r_.rs1.at[l, zb], r_.rsp_r.at[l, i, t % 2])
        both = r_.dxs[l, zb, par].astype(F32) + r_.rs1[l, zb].astype(F32)
        r_.cs[l, zb] = both.astype(BF16)
        send_rows(r_.cs.at[l, zb], r_.rs2.at[l, z], R, r_.rs_s.at[0], r_.rsc_r.at[l], nodes=2 * zb + par)

    def back_convolution(l, k):
        s0, g0 = unpack(jnp.sum(r_.st1[k + 1], 0))
        r_.gshift[l, 0:1] = s0
        r_.ggain[l, 0:1] = g0
        inv_den = 1.0 / (r_.den[l] + GATE_EPS)
        dm = r_.gain[l, 0:1] * r_.iv[l, 0:1] * (r_.gy0[...] - s0 / total - r_.z0[l] * (g0 / total))
        dnum = dm * inv_den
        dden = -dnum * r_.num[l] * inv_den
        high, low = split(jnp.concatenate([dnum, dden], 1))
        r_.dn[0:R] = high
        r_.dn[256 : 256 + R] = low
        r_.sc[0, 0:E, 0 : 2 * D] = dot(r_.le[:, 512:1024], r_.dn[...])
        for at in range(0, E, 64):
            here = slice(at, at + 64)
            gate, dnum_e = r_.gate[l, here], r_.sc[0, here, 0:D]
            dgp = (dnum_e * r_.bs[l, here].astype(F32) + r_.sc[0, here, D : 2 * D]) * gate * (1.0 - gate)
            r_.gg[here, 0:D] = (dnum_e * gate).astype(BF16)
            r_.gg[here, D:] = dgp.astype(BF16)
        ext = dot(r_.ST[...], r_.gg[0:E]).astype(BF16)
        r_.dproj[0:R, 0:D] = dm.astype(BF16)
        r_.dproj[:, D : 2 * D] = ext[:, 0:D]
        r_.dproj[0:R, 2 * D : 3 * D] = dot(r_.TT[:, 0:E], r_.gg[0:E, D:]).astype(BF16)
        r_.dproj[:, 3 * D :] = ext[:, D:]
        dxe = dot_nt(r_.dproj[...], r_.wp[l])
        r_.hs[l, 0] = dxe[R : R + 32].astype(BF16)
        r_.hs[l, 1] = dxe[R + 32 : R + 64].astype(BF16)
        r_.dxo[...] += dxe[0:R]

    def send_halo(l):
        send(r_.hs.at[l, 0], r_.hr.at[l, 1], r_.hal_s.at[0], r_.hal_r.at[l], nodes=prev)
        send(r_.hs.at[l, 1], r_.hr.at[l, 0], r_.hal_s.at[0], r_.hal_r.at[l], nodes=nxt)

    def conv_weight_grads(l):
        at = put(r_.gs_conv, l, 0, dot(r_.xeT[...], r_.dproj[...]))
        put(r_.gs_conv, l, at, dot(r_.efT[...], r_.gg[0:E, D:]))

    def back_input(l):
        dx = r_.dxo[...]
        dx = dx + r_.dxs[l, z, par].astype(F32)
        arrive(r_.ro.at[l], r_.ro_r.at[l])
        for slot in range(3):
            dx = dx + r_.ro[l, slot].astype(F32)
        if NZ > 2:
            arrive(r_.rs2.at[l, 0 : NZ - 2], r_.rsc_r.at[l])
        for t in range(2, NZ):
            dx = dx + r_.rs2[l, z_from(t)].astype(F32)
        arrive(r_.hr.at[l], r_.hal_r.at[l])
        back = jnp.concatenate(
            [r_.hr[l, 0].astype(F32)[0:24], r_.hr[l, 1].astype(F32)[0:24], jnp.zeros((16, D), F32)], 0
        )
        return dx + dot(r_.A[...], back.astype(BF16))

    r_.dy[...] = r_.cot[...].astype(F32)

    E1, C1, Q1, E0, C0, QK0, V0 = range(len(GROUPS))

    def steps(*pairs):
        return [functools.partial(reduce_step, g, k) for g, k in pairs]

    r_.dy[...] = r_.cot[...].astype(F32)

    def backward(b):
        l = L - 1 - b
        first, last = b == 0, b == L - 1
        k = 3 * L + 1 + 2 * b
        back_feed_forward(l, k)
        when(last, *steps((E1, 3), (Q1, 2)))
        back_norms(l, k)
        if first:
            when(True, *steps((E1, 0)))
            back_heads(l, 0, 0)
            back_heads(l, 0, 1)
            back_rows(l, 0)
            when(True, *steps((E1, 1)))
            sync_wait(k + 1)
            back_convolution(l, k)
            send_halo(l)
            pass_on(l, 0, 2)
            back_heads(l, 1, 0)
            pass_on(l, 0, 3)
            back_heads(l, 1, 1)
            back_rows(l, 1)
            conv_weight_grads(l)
            when(True, *steps((C1, 0)))
        else:
            when(True, *steps((C1, 3), (E1, 4), (E0, 0)))
            sync_wait(k + 1)
            back_convolution(l, k)
            send_halo(l)
            conv_weight_grads(l)
            when(True, *steps((E0, 1), (C0, 0)))
            back_heads(l, 0, 0)
            when(True, *steps((Q1, 3), (E1, 5), (C1, 4)))
            back_heads(l, 0, 1)
            back_rows(l, 0)
            when(True, *steps((E0, 2), (C0, 1), (Q1, 4), (E1, 6), (C1, 5)))
            back_heads(l, 1, 0)
            when(True, *steps((E0, 3), (Q1, 5), (C1, 6)))
            for t in range(2, NZ):
                pass_on(l, 0, t)
            back_heads(l, 1, 1)
            back_rows(l, 1)
            when(True, *steps((C0, 2), (E0, 4), (Q1, 6)))
        dqb = (r_.dqT[...].T * scale).astype(BF16)
        r_.dxo[...] += dot_nt(dqb, r_.wqkv[l, :, 0:D])
        at = put(r_.gs_qkv, l, 0, dot(r_.xeT[:, 0:R], dqb))
        put(r_.gs_qkv, l, at, r_.gkv[...].T)
        if first:
            when(True, *steps((Q1, 0), (C1, 1)))
            dx = back_input(l)
            r_.dy[...] = dx
            below = L - 2
            sync_start(SYNCS - 1, col_sum(dx), col_sum(dx * r_.z2[below]))
            when(True, *steps((E1, 2), (Q1, 1)))
            s2, g2 = sync_sums(SYNCS - 1)
            r_.gshift[below, 2:3] = s2
            r_.ggain[below, 2:3] = g2
            when(True, *steps((C1, 2)))

    for b in range(L):
        backward(b)
    for step in steps((QK0, 0), (V0, 0), (C0, 3), (E0, 5), (V0, 1), (QK0, 1)):
        step()
    r_.dy[...] = back_input(0)
    in_copy = pltpu.make_async_copy(r_.dy, r_.grad_in, r_.store.at[1])
    in_copy.start()
    for step in steps(
        (C0, 4), (E0, 6), (V0, 2), (QK0, 2),
        (C0, 5), (V0, 3), (QK0, 3),
        (C0, 6), (V0, 4), (QK0, 4),
    ):
        step()
    for l in range(L):
        for k in range(3):
            r_.ggain_out[k, l : l + 1] = r_.ggain[l, k : k + 1]
            r_.gshift_out[k, l : l + 1] = r_.gshift[l, k : k + 1]
    for g in range(len(GROUPS)):
        reduce_drain(g)
    sent(r_.meta.at[0 : N - 1], r_.meta_s.at[0])
    sent(r_.st1.at[:, 0 : M * N - 1], r_.st_s.at[0])
    sent(r_.gb.at[:, 0 : 3 + 2 * (NZ - 2)], r_.ag_s.at[0])
    sent(r_.gb.at[:, 0 : 2 * (NB - 1) + 3 + NZ - 2], r_.rs_s.at[0])
    sent(r_.hs, r_.hal_s.at[0])
    sent(r_.hx, r_.hx_s.at[0])
    act_copy.wait()
    in_copy.wait()


def finish_kernel(act_h, gin_h, *refs):
    n = len(GROUPS)
    held, (ggain_h, gshift_h), refs = refs[:n], refs[n : n + 2], refs[n + 2 :]
    act_o, gin_o, proj_o, edge_o, qkv_o, out_o, up_o, down_o, ggain_o, gshift_o = refs[:10]
    summed, refs = refs[10 : 10 + n], refs[10 + n :]
    act, gin, proj, edge, qkv, out, up, down, in_sem, out_sem = refs
    loads = [
        pltpu.make_async_copy(src, dst, in_sem.at[i])
        for i, (src, dst) in enumerate(zip(held + (act_h, gin_h), summed + (act, gin), strict=True))
    ]
    for load in loads:
        load.start()
    ggain_o[...] = ggain_h[...]
    gshift_o[...] = gshift_h[...]
    stores = []

    def store(src, dst):
        half = src.shape[0] // 2
        for rows in (pl.ds(0, half), pl.ds(half, half)):
            copy = pltpu.make_async_copy(src.at[rows], dst.at[rows], out_sem.at[len(stores)])
            copy.start()
            stores.append(copy)

    def widen(dst, l, g, at, first=0, last=None):
        rows = dst.shape[1]
        for c in range(first, dst.shape[2] // 128 if last is None else last):
            dst[l, :, 128 * c : 128 * (c + 1)] = summed[g][at : at + rows].astype(F32)
            at += rows
        return at

    for g, (name, l, first, rows, _) in enumerate(GROUPS):
        loads[g].wait()
        if name == "early":
            at = widen(out, l, g, 0)
            store(out.at[l], out_o.at[l])
            at = widen(up, l, g, at)
            store(up.at[l], up_o.at[l])
            widen(down, l, g, at)
            store(down.at[l], down_o.at[l])
        elif name == "conv":
            at = widen(proj, l, g, 0)
            store(proj.at[l], proj_o.at[l])
            widen(edge, l, g, at)
            store(edge.at[l], edge_o.at[l])
        else:
            widen(qkv, l, g, 0, first // 256, (first + rows) // 256)
            if first + rows == 1536:
                store(qkv.at[l], qkv_o.at[l])
    for i, (src, dst) in enumerate(((act, act_o), (gin, gin_o))):
        loads[n + i].wait()
        store(src, dst)
    for copy in stores:
        copy.wait()


def fused_device(
    N, M, node_input, edge_feat, graph_ids, edge_src, edge_dst, halo_send, w_proj, w_edge, w_qkv,
    w_out, w_up, w_down, norm_gain, norm_shift, cotangent,
):
    R, D = node_input.shape
    E = edge_feat.shape[0]
    L = w_proj.shape[0]
    names = scratch_list(N, M, L, R, E)
    vmem = pl.BlockSpec(memory_space=pltpu.VMEM)
    hbm = pl.BlockSpec(memory_space=pltpu.HBM)
    shape = jax.ShapeDtypeStruct
    rows = shape((R, D), F32)
    norm = shape((3, L, D), F32)
    groups = [shape((rows_g, 128), BF16) for _, _, _, rows_g, _ in GROUPS]
    outs = pl.pallas_call(
        functools.partial(kernel, N, M, L, tuple(names)),
        out_shape=[rows, rows, *groups, norm, norm],
        in_specs=[hbm] + [vmem] * 4 + [hbm] * 7 + [vmem] * 2 + [hbm],
        out_specs=[hbm] * (2 + len(GROUPS)) + [vmem] * 2,
        scratch_shapes=list(names.values()),
        compiler_params=pltpu.CompilerParams(
            collective_id=0, has_side_effects=True, vmem_limit_bytes=60 << 20
        ),
        name="layers",
    )(node_input, graph_ids, edge_src, edge_dst, halo_send, edge_feat, w_proj, w_edge, w_qkv, w_out, w_up,
      w_down, norm_gain.transpose(1, 0, 2), norm_shift.transpose(1, 0, 2), cotangent)
    weights = [shape(w.shape, F32) for w in (w_proj, w_edge, w_qkv, w_out, w_up, w_down)]
    results = pl.pallas_call(
        finish_kernel,
        out_shape=[rows, rows, *weights, norm, norm],
        in_specs=[hbm] * (2 + len(GROUPS)) + [vmem] * 2,
        out_specs=[hbm] * 8 + [vmem] * 2,
        scratch_shapes=[pltpu.VMEM(s.shape, s.dtype) for s in (*groups, rows, rows, *weights)]
        + [pltpu.SemaphoreType.DMA((len(GROUPS) + 2,)), pltpu.SemaphoreType.DMA((28,))],
        compiler_params=pltpu.CompilerParams(vmem_limit_bytes=60 << 20),
        name="gradients",
    )(*outs)
    ggain, gshift = results[8].transpose(1, 0, 2), results[9].transpose(1, 0, 2)
    return (*results[:8], ggain, gshift)


BLOCK_CAP = 2048


def extended_2(block, sides, width):
    for axis, dim in sides:
        count = lax.axis_size(axis)
        forward = [(i, i + 1) for i in range(count - 1)]
        forward.append((count - 1, 0))
        backward = [(target, source) for source, target in forward]
        low = lax.ppermute(
            lax.slice_in_dim(block, block.shape[dim] - width, None, axis=dim), axis, forward
        )
        high = lax.ppermute(lax.slice_in_dim(block, 0, width, axis=dim), axis, backward)
        block = jnp.concatenate([low, block, high], axis=dim)
    return block


def block_length(total_rows, upper_limit):
    for length in range(min(total_rows, upper_limit), 0, -1):
        if total_rows % length == 0:
            return length
    return 1


def outer_product(left, right):
    return lax.dot_general(
        left, right, (((0,), (0,)), ((), ())), preferred_element_type=jnp.float32
    )


def times_transposed(left, weight):
    return lax.dot_general(
        left, weight, (((1,), (1,)), ((), ())), preferred_element_type=jnp.float32
    )


def forward_product(left, weight):
    return jnp.dot(left, weight, preferred_element_type=jnp.float32)


def silu_slope_plain(inputs):
    logistic = jax.nn.sigmoid(inputs)
    return logistic * (1.0 + inputs * (1.0 - logistic))


def normalize(inputs, gain_row, shift_row, node_total):
    batch_mean = lax.psum(jnp.sum(inputs, 0), ("nodes", "rep")) / node_total
    centred = inputs - batch_mean
    batch_var = lax.psum(jnp.sum(centred * centred, 0), ("nodes", "rep")) / node_total
    inv_std = lax.rsqrt(batch_var + NORM_EPS)
    standard = (inputs - batch_mean) * inv_std
    return (standard * gain_row + shift_row, standard, inv_std)


def normalize_back(grad_out, standard, inv_std, gain_row, node_total):
    shift_grad, gain_grad = lax.psum(
        (jnp.sum(grad_out, 0), jnp.sum(grad_out * standard, 0)), ("nodes", "rep")
    )
    grad_in = (
        gain_row
        * inv_std
        * (grad_out - shift_grad / node_total - standard * gain_grad / node_total)
    )
    return (grad_in, gain_grad, shift_grad)


def exchange_sources(outgoing):
    halo_rows = outgoing.shape[0] // 2
    grown = extended_2(outgoing, (("nodes", 0),), halo_rows)
    return jnp.concatenate([grown[:halo_rows], grown[3 * halo_rows :]], 0)


def return_sources(incoming_grad):
    halo_rows = incoming_grad.shape[0] // 2
    grown = extended_2(incoming_grad.astype(jnp.bfloat16), (("nodes", 0),), halo_rows).astype(
        incoming_grad.dtype
    )
    return jnp.concatenate([grown[:halo_rows], grown[3 * halo_rows :]], 0)


def attend_forward(query_rows, key_rows, value_rows, local_graphs, group_graphs):
    row_count = query_rows.shape[0]
    score_scale = HEAD_DIM ** (-0.5)
    queries = query_rows.reshape(row_count, HEADS, HEAD_DIM)

    def add_piece(carried, kv_piece, first_row):
        key_piece, value_piece = kv_piece
        piece_rows = key_piece.shape[0]
        block_len = block_length(piece_rows, BLOCK_CAP)

        def add_block(block_state, block_index):
            row_max, row_sum, accumulated = block_state
            block_start = block_index * block_len
            key_block = lax.dynamic_slice_in_dim(key_piece, block_start, block_len, 0).reshape(
                block_len, HEADS, HEAD_DIM
            )
            value_block = lax.dynamic_slice_in_dim(value_piece, block_start, block_len, 0).reshape(
                block_len, HEADS, HEAD_DIM
            )
            key_graphs = lax.dynamic_slice_in_dim(
                group_graphs, first_row + block_start, block_len, 0
            )
            same_graph = (local_graphs[:, None] == key_graphs[None, :])[None]
            scores = (
                jnp.einsum("qhd,khd->hqk", queries, key_block, preferred_element_type=jnp.float32)
                * score_scale
            )
            scores = jnp.where(same_graph, scores, NEG)
            new_max = jnp.maximum(row_max, jnp.max(scores, 2))
            weights = jnp.where(same_graph, jnp.exp(scores - new_max[:, :, None]), 0.0)
            factor = jnp.exp(row_max - new_max)
            row_sum = row_sum * factor + jnp.sum(weights, 2)
            contrib = jnp.einsum(
                "hqk,khd->qhd",
                weights.astype(jnp.bfloat16),
                value_block,
                preferred_element_type=jnp.float32,
            )
            accumulated = accumulated * jnp.transpose(factor)[:, :, None] + contrib
            return ((new_max, row_sum, accumulated), None)

        carried, _ = lax.scan(add_block, carried, jnp.arange(piece_rows // block_len))
        return carried

    start_state = (
        jnp.full((HEADS, row_count), NEG, jnp.float32),
        jnp.zeros((HEADS, row_count), jnp.float32),
        jnp.zeros((row_count, HEADS, HEAD_DIM), jnp.float32),
    )
    row_max, row_sum, accumulated = add_piece(
        start_state,
        (
            lax.all_gather(key_rows, "nodes", axis=0, tiled=True),
            lax.all_gather(value_rows, "nodes", axis=0, tiled=True),
        ),
        jnp.int32(0),
    )
    attn_raw = accumulated / jnp.transpose(row_sum)[:, :, None]
    log_sum = row_max + jnp.log(row_sum)
    return (attn_raw, log_sum)


def attend_backward(
    query_rows, key_rows, value_rows, grad_low, attn_raw, log_sum, local_graphs, group_graphs
):
    row_count = query_rows.shape[0]
    model_width = HEADS * HEAD_DIM
    score_scale = HEAD_DIM ** (-0.5)
    queries = query_rows.reshape(row_count, HEADS, HEAD_DIM)
    grad_heads = grad_low.reshape(row_count, HEADS, HEAD_DIM)
    row_delta = jnp.einsum("qhd,qhd->hq", grad_heads.astype(jnp.float32), attn_raw)

    def score_block(key_block, value_block, key_graphs):
        same_graph = (local_graphs[:, None] == key_graphs[None, :])[None]
        scores = (
            jnp.einsum("qhd,khd->hqk", queries, key_block, preferred_element_type=jnp.float32)
            * score_scale
        )
        attn_weights = jnp.exp(jnp.where(same_graph, scores - log_sum[:, :, None], NEG))
        grad_weights = jnp.einsum(
            "qhd,khd->hqk", grad_heads, value_block, preferred_element_type=jnp.float32
        )
        grad_scores = (attn_weights * (grad_weights - row_delta[:, :, None])).astype(jnp.bfloat16)
        return (attn_weights, grad_scores)

    def key_terms(attn_weights, grad_scores, block_len):
        grad_keys = (
            jnp.einsum("hqk,qhd->khd", grad_scores, queries, preferred_element_type=jnp.float32)
            * score_scale
        )
        grad_values = jnp.einsum(
            "hqk,qhd->khd",
            attn_weights.astype(jnp.bfloat16),
            grad_heads,
            preferred_element_type=jnp.float32,
        )
        return jnp.concatenate(
            [
                grad_keys.reshape(block_len, model_width),
                grad_values.reshape(block_len, model_width),
            ],
            1,
        )

    def query_term(grad_scores, key_block):
        return (
            jnp.einsum("hqk,khd->qhd", grad_scores, key_block, preferred_element_type=jnp.float32)
            * score_scale
        )

    group_rows = group_graphs.shape[0]

    def add_piece(carried, kv_piece, first_row):
        key_piece, value_piece = kv_piece
        piece_rows = key_piece.shape[0]
        block_len = block_length(piece_rows, BLOCK_CAP)

        def add_block(block_state, block_index):
            grad_query, buffer = block_state
            block_start = block_index * block_len
            key_block = lax.dynamic_slice_in_dim(key_piece, block_start, block_len, 0).reshape(
                block_len, HEADS, HEAD_DIM
            )
            value_block = lax.dynamic_slice_in_dim(value_piece, block_start, block_len, 0).reshape(
                block_len, HEADS, HEAD_DIM
            )
            place = first_row + block_start
            key_graphs = lax.dynamic_slice_in_dim(group_graphs, place, block_len, 0)
            attn_weights, grad_scores = score_block(key_block, value_block, key_graphs)
            grad_query = grad_query + query_term(grad_scores, key_block)
            block_terms = key_terms(attn_weights, grad_scores, block_len)
            current = lax.dynamic_slice_in_dim(buffer, place, block_len, 0)
            buffer = lax.dynamic_update_slice_in_dim(buffer, current + block_terms, place, 0)
            return ((grad_query, buffer), None)

        carried, _ = lax.scan(add_block, carried, jnp.arange(piece_rows // block_len))
        return carried

    start_state = (
        jnp.zeros((row_count, HEADS, HEAD_DIM), jnp.float32),
        jnp.zeros((group_rows, 2 * model_width), jnp.float32),
    )
    grad_query, buffer = add_piece(
        start_state,
        (
            lax.all_gather(key_rows, "nodes", axis=0, tiled=True),
            lax.all_gather(value_rows, "nodes", axis=0, tiled=True),
        ),
        jnp.int32(0),
    )
    grad_kv = lax.psum_scatter(buffer, "nodes", scatter_dimension=0, tiled=True)
    return (
        grad_query.reshape(row_count, model_width),
        grad_kv[:, :model_width],
        grad_kv[:, model_width:],
    )


def layer_forward(
    hidden, params, edge_feat, edge_src, edge_dst, halo_send, local_graphs, group_graphs, node_total
):
    w_proj, w_edge, w_qkv, w_out, w_up, w_down, norm_gains, norm_shifts = params
    row_count, model_width = hidden.shape
    hidden_low = hidden.astype(jnp.bfloat16)
    projected = forward_product(hidden_low, w_proj)
    self_term = projected[:, :model_width]
    dest_term = projected[:, 2 * model_width : 3 * model_width]
    source_rows = jnp.concatenate(
        [projected[:, model_width : 2 * model_width], projected[:, 3 * model_width :]], 1
    ).astype(jnp.bfloat16)
    incoming = exchange_sources(source_rows[halo_send])
    extended = jnp.concatenate([source_rows, incoming], 0)
    edge_rows = extended[edge_src].astype(jnp.float32)
    source_b = edge_rows[:, :model_width]
    source_e = edge_rows[:, model_width:]
    edge_proj = forward_product(edge_feat, w_edge)
    gating = jax.nn.sigmoid(dest_term[edge_dst] + source_e + edge_proj)
    numerator = jax.ops.segment_sum(gating * source_b, edge_dst, row_count)
    denominator = jax.ops.segment_sum(gating, edge_dst, row_count)
    message = self_term + numerator / (denominator + GATE_EPS)
    normed_one, standard_one, inv_one = normalize(
        message, norm_gains[0], norm_shifts[0], node_total
    )
    local_out = hidden + jax.nn.silu(normed_one)
    qkv_low = forward_product(hidden_low, w_qkv).astype(jnp.bfloat16)
    query_rows = qkv_low[:, :model_width]
    key_rows = qkv_low[:, model_width : 2 * model_width]
    value_rows = qkv_low[:, 2 * model_width :]
    attn_raw, log_sum = attend_forward(query_rows, key_rows, value_rows, local_graphs, group_graphs)
    attn_low = attn_raw.reshape(row_count, model_width).astype(jnp.bfloat16)
    attn_proj = forward_product(attn_low, w_out)
    normed_two, standard_two, inv_two = normalize(
        hidden + attn_proj, norm_gains[1], norm_shifts[1], node_total
    )
    mixed = local_out + normed_two
    mixed_low = mixed.astype(jnp.bfloat16)
    up_proj = forward_product(mixed_low, w_up)
    activated = jax.nn.silu(up_proj).astype(jnp.bfloat16)
    down_proj = forward_product(activated, w_down)
    normed_three, standard_three, inv_three = normalize(
        mixed + down_proj, norm_gains[2], norm_shifts[2], node_total
    )
    saved = (
        hidden_low,
        source_b,
        gating,
        numerator,
        denominator,
        normed_one,
        standard_one,
        inv_one,
        query_rows,
        key_rows,
        value_rows,
        attn_raw,
        log_sum,
        attn_low,
        standard_two,
        inv_two,
        mixed_low,
        up_proj,
        activated,
        standard_three,
        inv_three,
    )
    return (normed_three, saved)


def layer_backward(
    grad_out,
    params,
    saved,
    edge_feat,
    edge_src,
    edge_dst,
    halo_send,
    local_graphs,
    group_graphs,
    node_total,
):
    w_proj, w_edge, w_qkv, w_out, w_up, w_down, norm_gains, norm_shifts = params
    (
        hidden_low,
        source_b,
        gating,
        numerator,
        denominator,
        normed_one,
        standard_one,
        inv_one,
        query_rows,
        key_rows,
        value_rows,
        attn_raw,
        log_sum,
        attn_low,
        standard_two,
        inv_two,
        mixed_low,
        up_proj,
        activated,
        standard_three,
        inv_three,
    ) = saved
    row_count, model_width = grad_out.shape
    grad_three, gain_three, shift_three = normalize_back(
        grad_out, standard_three, inv_three, norm_gains[2], node_total
    )
    down_grad = grad_three.astype(jnp.bfloat16)
    grad_w_down = outer_product(activated, down_grad)
    up_grad = (times_transposed(down_grad, w_down) * silu_slope_plain(up_proj)).astype(jnp.bfloat16)
    grad_w_up = outer_product(mixed_low, up_grad)
    grad_mixed = grad_three + times_transposed(up_grad, w_up)
    grad_two, gain_two, shift_two = normalize_back(
        grad_mixed, standard_two, inv_two, norm_gains[1], node_total
    )
    out_grad = grad_two.astype(jnp.bfloat16)
    grad_w_out = outer_product(attn_low, out_grad)
    attn_grad = times_transposed(out_grad, w_out).astype(jnp.bfloat16)
    grad_query, grad_key, grad_value = attend_backward(
        query_rows, key_rows, value_rows, attn_grad, attn_raw, log_sum, local_graphs, group_graphs
    )
    qkv_grad = jnp.concatenate([grad_query, grad_key, grad_value], 1).astype(jnp.bfloat16)
    grad_w_qkv = outer_product(hidden_low, qkv_grad)
    grad_message, gain_one, shift_one = normalize_back(
        grad_mixed * silu_slope_plain(normed_one), standard_one, inv_one, norm_gains[0], node_total
    )
    shifted = denominator + GATE_EPS
    grad_numer = grad_message / shifted
    grad_denom = -grad_message * numerator / (shifted * shifted)
    numer_edge = grad_numer[edge_dst]
    grad_gate = numer_edge * source_b + grad_denom[edge_dst]
    grad_pre_edge = grad_gate * gating * (1.0 - gating)
    edge_grad = grad_pre_edge.astype(jnp.bfloat16)
    grad_w_edge = outer_product(edge_feat, edge_grad)
    grad_dest = jax.ops.segment_sum(grad_pre_edge, edge_dst, row_count)
    grad_extended = jax.ops.segment_sum(
        jnp.concatenate([numer_edge * gating, grad_pre_edge], 1),
        edge_src,
        row_count + halo_send.shape[0],
    )
    returned = return_sources(grad_extended[row_count:])
    grad_source = grad_extended[:row_count].at[halo_send].add(returned)
    proj_grad = jnp.concatenate(
        [grad_message, grad_source[:, :model_width], grad_dest, grad_source[:, model_width:]], 1
    ).astype(jnp.bfloat16)
    grad_w_proj = outer_product(hidden_low, proj_grad)
    grad_hidden = (
        grad_mixed
        + grad_two
        + times_transposed(proj_grad, w_proj)
        + times_transposed(qkv_grad, w_qkv)
    )
    weight_grads = (grad_w_proj, grad_w_edge, grad_w_qkv, grad_w_out, grad_w_up, grad_w_down)
    return (
        grad_hidden,
        weight_grads,
        jnp.stack([gain_one, gain_two, gain_three]),
        jnp.stack([shift_one, shift_two, shift_three]),
    )


def per_device(
    node_input,
    edge_feat,
    graph_ids,
    edge_src,
    edge_dst,
    halo_send,
    w_proj,
    w_edge,
    w_qkv,
    w_out,
    w_up,
    w_down,
    norm_gain,
    norm_shift,
    cotangent,
):
    group_graphs = lax.all_gather(graph_ids, "nodes", axis=0, tiled=True)
    node_total = node_input.shape[0] * lax.axis_size("nodes") * lax.axis_size("rep")
    layer_count = w_proj.shape[0]
    layer_params = [
        (
            w_proj[layer_index],
            w_edge[layer_index],
            w_qkv[layer_index],
            w_out[layer_index],
            w_up[layer_index],
            w_down[layer_index],
            norm_gain[layer_index],
            norm_shift[layer_index],
        )
        for layer_index in range(layer_count)
    ]
    hidden = node_input.astype(jnp.float32)
    saved_all = []
    for layer_index in range(layer_count):
        hidden, saved = layer_forward(
            hidden,
            layer_params[layer_index],
            edge_feat,
            edge_src,
            edge_dst,
            halo_send,
            graph_ids,
            group_graphs,
            node_total,
        )
        saved_all.append(saved)
    grad_hidden = cotangent.astype(jnp.float32)
    weight_parts = [None] * layer_count
    gain_parts = [None] * layer_count
    shift_parts = [None] * layer_count
    for layer_index in range(layer_count - 1, -1, -1):
        (
            grad_hidden,
            weight_parts[layer_index],
            gain_parts[layer_index],
            shift_parts[layer_index],
        ) = layer_backward(
            grad_hidden,
            layer_params[layer_index],
            saved_all[layer_index],
            edge_feat,
            edge_src,
            edge_dst,
            halo_send,
            graph_ids,
            group_graphs,
            node_total,
        )
    proj_local = jnp.stack([weight_parts[layer_index][0] for layer_index in range(layer_count)])
    edge_local = jnp.stack([weight_parts[layer_index][1] for layer_index in range(layer_count)])
    qkv_local = jnp.stack([weight_parts[layer_index][2] for layer_index in range(layer_count)])
    out_local = jnp.stack([weight_parts[layer_index][3] for layer_index in range(layer_count)])
    up_local = jnp.stack([weight_parts[layer_index][4] for layer_index in range(layer_count)])
    down_local = jnp.stack([weight_parts[layer_index][5] for layer_index in range(layer_count)])
    grad_proj, grad_edge, grad_qkv, grad_out, grad_up, grad_down = lax.psum(
        (proj_local, edge_local, qkv_local, out_local, up_local, down_local), ("nodes", "rep")
    )
    return (
        hidden,
        grad_hidden,
        grad_proj,
        grad_edge,
        grad_qkv,
        grad_out,
        grad_up,
        grad_down,
        jnp.stack(gain_parts),
        jnp.stack(shift_parts),
    )


def solution(mesh):
    in_specs = (
        P(("rep", "nodes"), None),
        P(("rep", "nodes"), None),
        P(("rep", "nodes")),
        P(("rep", "nodes")),
        P(("rep", "nodes")),
        P(("rep", "nodes")),
        P(),
        P(),
        P(),
        P(),
        P(),
        P(),
        P(),
        P(),
        P(("rep", "nodes"), None),
    )
    out_specs = (
        P(("rep", "nodes"), None),
        P(("rep", "nodes"), None),
        P(),
        P(),
        P(),
        P(),
        P(),
        P(),
        P(),
        P(),
    )
    N, M = mesh.shape["nodes"], mesh.shape["rep"]
    fused = N in (4, 8) and M % 2 == 0 and 512 % (16 * N * M) == 0
    return jax.shard_map(
        functools.partial(fused_device, N, M) if fused else per_device,
        mesh=mesh, in_specs=in_specs, out_specs=out_specs, check_vma=False,
    )
```

```python
import functools
import math

import jax
import jax.numpy as jnp
from jax import lax
from jax.experimental import pallas as pl
from jax.experimental.pallas import tpu as pltpu
from jax.sharding import PartitionSpec as P

HEADS = 8
HEAD_DIM = 32
NEG = -1e30
NORM_EPS = 1e-05
GATE_EPS = 1e-06
F32, BF16, I32 = jnp.float32, jnp.bfloat16, jnp.int32
MESH = pl.DeviceIdType.MESH
SYNCS = 12
STRIP = 32
GROUPS = (
    ("early", 1, 0, 2560, ("core", "y", "x", "z")),
    ("conv", 1, 0, 2560, ("core", "y", "x", "z")),
    ("qkv", 1, 0, 1536, ("core", "y", "x", "z")),
    ("early", 0, 0, 2560, ("core", "x", "y", "z")),
    ("conv", 0, 0, 2560, ("core", "y", "x", "z")),
    ("qkv", 0, 0, 1024, ("rep", "nodes")),
    ("qkv", 0, 1024, 512, ("nodes", "rep")),
)


def dot(left, right):
    return lax.dot_general(
        left, right, (((1,), (0,)), ((), ())), preferred_element_type=F32
    )


def dot_nt(left, right):
    return lax.dot_general(
        left, right, (((1,), (1,)), ((), ())), preferred_element_type=F32
    )


def dot_tn(left, right):
    return lax.dot_general(
        left, right, (((0,), (0,)), ((), ())), preferred_element_type=F32
    )


def split(value):
    high = value.astype(BF16)
    return high, (value - high.astype(F32)).astype(BF16)


def sigmoid(value):
    return jax.nn.sigmoid(value)


def silu_slope(value):
    logistic = sigmoid(value)
    return logistic * (1.0 + value * (1.0 - logistic))


def col_sum(value):
    return jnp.sum(value, axis=0, keepdims=True)


def pack(first, second):
    return jnp.concatenate([first[:, :128], first[:, 128:], second[:, :128], second[:, 128:]], 0)


def unpack(tile):
    return [jnp.concatenate([tile[i : i + 1], tile[i + 1 : i + 2]], 1) for i in (0, 2)]


def combine_moments(tiles, count):
    mean = jnp.mean(tiles[:, 0:2], 0)
    off = tiles[:, 0:2] - mean
    return jnp.concatenate([mean, jnp.sum(tiles[:, 2:4] + count * off * off, 0)], 0)


class Refs:
    pass


def axis_sizes(N, M):
    return dict(core=2, y=M // 2, x=2, z=N // 2, rep=M, nodes=N)


def scratch_list(N, M, L, R, E):
    NZ, NB, G = N // 2, N // 4, N * R
    D, FF, W, HH = 256, 512, 4 * R, HEADS // 2 * R
    dma = lambda *shape: pltpu.SemaphoreType.DMA(shape)
    vm = lambda dtype, *shape: pltpu.VMEM(shape, dtype)
    names = dict(
        gb=vm(BF16, L, N, R, D),
        xs=vm(BF16, L, N, R, D),
        meta=vm(I32, N, 8, 256),
        cot=vm(BF16, R, D),
        wp=vm(BF16, L, D, 4 * D),
        we=vm(BF16, L, D, D),
        wqkv=vm(BF16, L, D, 3 * D),
        wo=vm(BF16, L, D, D),
        wu=vm(BF16, L, D, FF),
        wd=vm(BF16, L, FF, D),
        st1=vm(F32, SYNCS, M * N, 4, 128),
        gain=vm(F32, L, 8, D),
        shift=vm(F32, L, 8, D),
        ggain=vm(F32, L, 8, D),
        gshift=vm(F32, L, 8, D),
        iv=vm(F32, L, 8, D),
        moff=vm(F32, N, 8, D),
        move=vm(F32, 8, D),
        le=vm(BF16, E, 1024),
        re=vm(BF16, 1024, D),
        TT=vm(BF16, R, 2 * E),
        ST=vm(BF16, 256, E),
        efT=vm(BF16, D, E),
        HS=vm(BF16, 64, R),
        hx=vm(BF16, L, 64, D),
        A=vm(BF16, R, 64),
        bias=vm(F32, R, G),
        xf=vm(F32, L + 1, R, D),
        xe=vm(BF16, L, 256, D),
        xeT=vm(BF16, D, 256),
        gate=vm(F32, L, E, D),
        bs=vm(BF16, L, E, D),
        num=vm(F32, L, R, D),
        den=vm(F32, L, R, D),
        z0=vm(F32, L, R, D),
        z1=vm(F32, L, R, D),
        z2=vm(F32, L, R, D),
        wkvT=vm(BF16, L, 2 * D, D),
        kvT=vm(BF16, L, 2 * D, G),
        odT=vm(F32, NB, D, R),
        ldT=vm(F32, NB, D, R),
        md=vm(F32, NB, R, D),
        rb=vm(F32, L, NB, R, D),
        pst=vm(BF16, L, HEADS * R, G),
        oraw=vm(F32, L, R, D),
        ob=vm(BF16, L, R, D),
        mb=vm(BF16, L, R, D),
        u=vm(F32, L, R, FF),
        g=vm(BF16, L, R, FF),
        dy=vm(F32, R, D),
        dmix=vm(F32, R, D),
        gy0=vm(F32, R, D),
        local=vm(F32, R, D),
        dxo=vm(F32, R, D),
        dob=vm(F32, R, D),
        dqT=vm(F32, D, R),
        qm=vm(BF16, L, 2, HH, 128),
        q=vm(BF16, L, R, D),
        qT=vm(BF16, D, R),
        dosT=vm(BF16, 128, R),
        dom=vm(BF16, HH, 256),
        sc=vm(F32, 2, max(2 * R, E), W),
        tp=vm(F32, HEADS // 2, R, 128),
        dss=vm(BF16, HH, W),
        dkv=vm(BF16, 2 * D, W),
        gkv=vm(F32, 2 * D, D),
        gg=vm(BF16, 2 * E, 2 * D),
        dn=vm(BF16, 512, 2 * D),
        dproj=vm(BF16, 256, 4 * D),
        dxs=vm(BF16, L, NZ, 2, R, D),
        rs1=vm(BF16, L, NZ, R, D),
        cs=vm(BF16, L, NZ, R, D),
        rs2=vm(BF16, L, NZ, R, D),
        ro=vm(BF16, L, 3, R, D),
        hs=vm(BF16, L, 2, 32, D),
        hr=vm(BF16, L, 2, 32, D),
    )
    names.update(
        gs_early=vm(BF16, L, 2560, 128),
        gs_conv=vm(BF16, L, 2560, 128),
        gs_qkv=vm(BF16, L, 1536, 128),
    )
    sizes = axis_sizes(N, M)
    for g, (_, _, _, rows, stages) in enumerate(GROUPS):
        names[f"go{g}"] = vm(BF16, rows, 128)
        left = rows
        for k, axis in enumerate(stages):
            left //= sizes[axis]
            names[f"ga{g}_{k}"] = vm(BF16, sizes[axis] - 1, left, 128)
            if k < len(stages) - 1:
                names[f"gh{g}_{k}"] = vm(BF16, left, 128)
    names.update(
        ar_s=dma(len(GROUPS)),
        ar_r=dma(sum(2 * len(stages) for *_, stages in GROUPS)),
        ar_l=dma(len(GROUPS)),
        load=dma(9),
        store=dma(2),
        meta_s=dma(1),
        meta_r=dma(1),
        st_s=dma(1),
        st_r=dma(SYNCS),
        ag_s=dma(1),
        agn_r=dma(L),
        agc_r=dma(L, NZ),
        agp_r=dma(L),
        rs_s=dma(1),
        rsp_r=dma(L, NB, 2),
        ro_r=dma(L),
        rsc_r=dma(L),
        hx_s=dma(1),
        hx_r=dma(L),
        hal_s=dma(1),
        hal_r=dma(L),
    )
    return names


IN_NAMES = (
    "x_in", "ids", "edge_src", "edge_dst", "halo", "ef_h", "wp_h", "we_h", "wqkv_h", "wo_h", "wu_h", "wd_h",
    "gain_in", "shift_in", "cot_h",
)
OUT_NAMES = ("out_act", "grad_in", *(f"gout{g}" for g in range(len(GROUPS))), "ggain_out", "gshift_out")


def kernel(N, M, L, names, *args):
    r_ = Refs()
    for name, ref in zip(IN_NAMES + OUT_NAMES + tuple(names), args, strict=True):
        setattr(r_, name, ref)
    R, D = r_.x_in.shape
    E = r_.ef_h.shape[0]
    NZ, NB, G, W = N // 2, N // 4, N * R, 4 * R
    HK = HEADS // 2
    total = float(N * M * R)
    scale = HEAD_DIM ** -0.5
    me = lax.axis_index("nodes")
    rep = lax.axis_index("rep")
    z = me // 2
    par = me % 2
    partner = 2 * z + (1 - par)
    prev = (me + N - 1) % N
    nxt = (me + 1) % N
    zh, zl = z // 2, z % 2
    z_to = lambda t: 2 * ((zh + t // 2) % NB) + (zl + t % 2) % 2
    z_from = lambda t: 2 * ((zh + NB - t // 2) % NB) + (zl + t % 2) % 2

    def remote(src, dst, s_sem, r_sem, **where):
        return pltpu.make_async_remote_copy(
            src_ref=src, dst_ref=dst, send_sem=s_sem, recv_sem=r_sem,
            device_id=where, device_id_type=MESH,
        )

    def send(src, dst, s_sem, r_sem, **where):
        remote(src, dst, s_sem, r_sem, **where).start()

    def send_rows(src, dst, rows, s_sem, r_sem, **where):
        pieces = next(p for p in range(1, rows) if rows % (16 * p) == 0 and rows // p <= 128)
        for at in range(0, rows, rows // pieces):
            cut = pl.ds(at, rows // pieces)
            send(src.at[cut], dst.at[cut], s_sem, r_sem, **where)

    def arrive(dst, r_sem):
        remote(dst, dst, r_sem, r_sem, nodes=partner).wait_recv()

    def sent(src, s_sem):
        remote(src, src, s_sem, s_sem, nodes=partner).wait_send()

    def when(condition, *acts):
        if condition:
            for act in acts:
                act()

    loads = [pltpu.make_async_copy(r_.ef_h, r_.le.at[:, D : 2 * D], r_.load.at[0])] + [
        pltpu.make_async_copy(getattr(r_, f"{name}_h"), getattr(r_, name), r_.load.at[1 + i])
        for i, name in enumerate(("we", "wqkv", "wp", "wo", "wu", "wd", "cot"))
    ]
    own_rows = pltpu.make_async_copy(r_.x_in, r_.gb.at[0, me], r_.load.at[8])
    own_rows.start()
    for load in loads:
        load.start()

    barrier = pltpu.get_barrier_semaphore()
    for dr in range(M):
        for d in range(N):
            if dr + d > 0:
                pl.semaphore_signal(barrier, inc=1, device_id={"rep": (rep + dr) % M, "nodes": (me + d) % N},
                                    device_id_type=MESH)
    pl.semaphore_wait(barrier, M * N - 1)

    def gather_start(l):
        mine = r_.gb.at[l, me]
        for t in range(2, NZ):
            send_rows(mine, mine, R, r_.ag_s.at[0], r_.agc_r.at[l, t], nodes=2 * z_to(t) + par)
        send_rows(mine, mine, R, r_.ag_s.at[0], r_.agn_r.at[l], nodes=partner)
        send_rows(mine, mine, R, r_.ag_s.at[0], r_.agn_r.at[l], nodes=2 * z_to(1) + par)
        send_rows(mine, mine, R, r_.ag_s.at[0], r_.agn_r.at[l], nodes=2 * z_to(1) + 1 - par)

    def gather_pass(l, t):
        piece = r_.gb.at[l, 2 * z_from(t) + par]
        arrive(piece, r_.agc_r.at[l, t])
        send_rows(piece, piece, R, r_.ag_s.at[0], r_.agp_r.at[l], nodes=partner)

    def gather_near(l):
        arrive(r_.gb.at[l, 0:3], r_.agn_r.at[l])

    def gather_far(l):
        arrive(r_.gb.at[l, 0 : NZ - 2], r_.agp_r.at[l])

    def sync_start(k, first, second):
        mine = rep * N + me
        r_.st1[k, mine] = pack(first, second)
        for dr in range(M):
            for d in range(N):
                if dr + d > 0:
                    send(r_.st1.at[k, mine], r_.st1.at[k, mine], r_.st_s.at[0], r_.st_r.at[k],
                         rep=(rep + dr) % M, nodes=(me + d) % N)

    def sync_wait(k):
        arrive(r_.st1.at[k, 0 : M * N - 1], r_.st_r.at[k])

    def sync_moments(k):
        sync_wait(k)
        return unpack(combine_moments(r_.st1[k], float(R)))

    def sync_sums(k):
        sync_wait(k)
        return unpack(jnp.sum(r_.st1[k], 0))

    sizes = axis_sizes(N, M)
    core, row = rep % 2, rep // 2
    places = dict(
        core=(core, lambda t: dict(rep=2 * row + t)),
        y=(row, lambda t: dict(rep=2 * t + core)),
        x=(par, lambda t: dict(nodes=2 * z + t)),
        z=(z, lambda t: dict(nodes=2 * t + par)),
        rep=(rep, lambda t: dict(rep=t)),
        nodes=(me, lambda t: dict(nodes=t)),
    )

    def reduce_step(g, step):
        name, layer, first, rows, stages = GROUPS[g]
        K = len(stages)
        base = sum(2 * len(before) for *_, before in GROUPS[:g])
        gs, out = getattr(r_, f"gs_{name}").at[layer, first : first + rows], getattr(r_, f"go{g}")
        count, offset = [rows], [0]
        for axis in stages:
            count.append(count[-1] // sizes[axis])
            offset.append(offset[-1] + places[axis][0] * count[-1])
        take = lambda start, size: pl.ds(pl.multiple_of(start, 16), size)
        if 1 <= step <= K:
            k = step - 1
            got = getattr(r_, f"ga{g}_{k}")
            arrive(got, r_.ar_r.at[base + k])
            held = gs if k == 0 else getattr(r_, f"gh{g}_{k - 1}")
            index = places[stages[k]][0]
            acc = held[take(index * count[k + 1], count[k + 1])].astype(F32)
            for slot in range(sizes[stages[k]] - 1):
                acc = acc + got[slot].astype(F32)
            if step < K:
                getattr(r_, f"gh{g}_{k}")[...] = acc.astype(BF16)
            else:
                out[take(offset[K], count[K])] = acc.astype(BF16)
        elif step > K:
            k = 2 * K - step
            arrive(out.at[0 : (sizes[stages[k]] - 1) * count[k + 1]], r_.ar_r.at[base + step - 1])
        if step < K:
            held = gs if step == 0 else getattr(r_, f"gh{g}_{step - 1}")
            index, device = places[stages[step]]
            size = sizes[stages[step]]
            for d in range(1, size):
                to = (index + d) % size
                send_rows(held.at[take(to * count[step + 1], count[step + 1])], getattr(r_, f"ga{g}_{step}").at[d - 1],
                     count[step + 1], r_.ar_s.at[g], r_.ar_r.at[base + step], **device(to))
        elif step < 2 * K:
            k = 2 * K - 1 - step
            index, device = places[stages[k]]
            size = sizes[stages[k]]
            here = out.at[take(offset[k + 1], count[k + 1])]
            for d in range(1, size):
                send_rows(here, here, count[k + 1], r_.ar_s.at[g], r_.ar_r.at[base + step],
                          **device((index + d) % size))
        else:
            pltpu.make_async_copy(out, getattr(r_, f"gout{g}"), r_.ar_l.at[g]).start()

    def reduce_drain(g):
        name, _, _, rows, _ = GROUPS[g]
        sent(getattr(r_, f"gs_{name}").at[:, 0 : rows - rows // (M * N)], r_.ar_s.at[g])
        pltpu.make_async_copy(getattr(r_, f"go{g}"), getattr(r_, f"gout{g}"), r_.ar_l.at[g]).wait()

    def put(buf, l, at, value):
        rows = value.shape[0]
        for c in range(value.shape[1] // 128):
            buf[l, at : at + rows] = value[:, 128 * c : 128 * (c + 1)].astype(BF16)
            at += rows
        return at

    lane_head = lax.broadcasted_iota(I32, (R, 128), 1) // HEAD_DIM

    def by_head(parts):
        out = parts[0]
        for k in range(1, HK):
            out = jnp.where(lane_head == k, parts[k], out)
        return out

    r_.meta[me] = jnp.full((8, 256), -1, I32)
    r_.meta[me, 0:1, 0:R] = r_.ids[...].reshape(1, R)
    r_.meta[me, 1:2, 0:48] = r_.halo[...].reshape(1, 48)
    for d in range(1, N):
        send(r_.meta.at[me], r_.meta.at[me], r_.meta_s.at[0], r_.meta_r.at[0], nodes=(me + d) % N)
    own_rows.wait()
    gather_start(0)

    src_row = r_.edge_src[...].reshape(1, E)
    src_row = jnp.where(src_row < R + 24, src_row, src_row + 8)
    dst_row = r_.edge_dst[...].reshape(1, E)
    src_col = jnp.broadcast_to(src_row, (128, E)).T[:, 0:1]
    dst_col = jnp.broadcast_to(dst_row, (128, E)).T[:, 0:1]
    as_mask = lambda cond: cond.astype(F32).astype(BF16)
    r_.le[:, 0:256] = as_mask(src_col == lax.broadcasted_iota(I32, (E, 256), 1))
    target = as_mask(dst_col == lax.broadcasted_iota(I32, (E, 256), 1))
    r_.le[:, 512:768] = target
    r_.le[:, 768:1024] = target
    target = as_mask(dst_row == lax.broadcasted_iota(I32, (R, E), 0))
    r_.TT[:, 0:E] = target
    r_.TT[:, E:] = target
    r_.ST[...] = as_mask(src_row == lax.broadcasted_iota(I32, (256, E), 0))
    r_.dn[R:256] = jnp.zeros((256 - R, 2 * D), BF16)
    r_.dn[256 + R : 512] = jnp.zeros((256 - R, 2 * D), BF16)
    r_.dproj[R:256, 0:D] = jnp.zeros((256 - R, D), BF16)
    r_.dproj[R:256, 2 * D : 3 * D] = jnp.zeros((256 - R, D), BF16)
    halo_col = jnp.broadcast_to(r_.meta[me][1:2, 0:128], (128, 128)).T
    hot = (halo_col[0:48, 0:1] == lax.broadcasted_iota(I32, (48, R), 1)).astype(F32)
    pad = jnp.zeros((8, R), F32)
    r_.HS[...] = jnp.concatenate([hot[0:24], pad, hot[24:48], pad], 0).astype(BF16)
    loads[0].wait()
    r_.efT[...] = r_.le[:, D : 2 * D].T
    for l in range(L):
        for k in range(3):
            r_.gain[l, k : k + 1] = r_.gain_in[k, l : l + 1]
            r_.shift[l, k : k + 1] = r_.shift_in[k, l : l + 1]
    r_.xf[0] = r_.gb[0, me].astype(F32)
    r_.moff[...] = jnp.zeros((N, 8, D), F32)
    r_.move[0:1] = jnp.ones((1, D), F32)
    r_.move[1:2] = jnp.zeros((1, D), F32)
    for load in loads[1:]:
        load.wait()
    for l in range(L):
        r_.wkvT[l] = r_.wqkv[l, :, D:].T

    arrive(r_.meta.at[0 : N - 1], r_.meta_r.at[0])
    id_col = jnp.broadcast_to(r_.meta[me][0:1, 0:R], (128, R)).T[:, 0:1]
    id_row = jnp.concatenate(
        [r_.meta[4 * ((zh + NB - j // 4) % NB) + j % 4][0:1, 0:R] for j in range(N)], 1
    )
    r_.bias[...] = jnp.where(id_col == id_row, 0.0, NEG)

    r_.A[...] = as_mask(r_.meta[me][1:2, 0:64] == lax.broadcasted_iota(I32, (R, 64), 0))

    factor_exp = scale * math.log2(math.e)

    def prepare_queries(l):
        q = dot(r_.xs[l, me], r_.wqkv[l, :, :D]).astype(BF16)
        r_.q[l] = q
        q = q.astype(F32)
        for hf in range(2):
            for k in range(HK):
                part = jnp.where(lane_head == k, q[:, 128 * hf : 128 * (hf + 1)], 0.0)
                r_.qm[l, hf, k * R : (k + 1) * R] = part.astype(BF16)

    def head_dims(hf, k, base=0):
        first = base + hf * 128 + k * HEAD_DIM
        return slice(first, first + HEAD_DIM)

    def head_rows(hf, k, count=1):
        return slice((hf * HK + k) * R, (hf * HK + k + count) * R)

    def lane_half(hf):
        return slice(hf * 128, (hf + 1) * 128)

    def half_of(i):
        return (zh + NB - i) % NB, slice(i * W, (i + 1) * W)

    def attention_keys(l, i):
        half, rows = half_of(i)
        x = r_.xs[l, pl.ds(4 * half, 4)].reshape(W, D)
        r_.kvT[l, :, rows] = dot_nt(r_.wkvT[l], x).astype(BF16)

    def attention_heads(l, i, hfs):
        _, rows = half_of(i)
        for hf in hfs:
            lanes = lane_half(hf)
            ones = jnp.ones((HEAD_DIM, W), BF16)
            for c in range(HK // 2):
                r_.sc[c % 2, 0 : 2 * R] = dot(r_.qm[l, hf, 2 * c * R : 2 * (c + 1) * R], r_.kvT[l, lanes, rows])
                for k in range(2):
                    for at in range(0, R, STRIP):
                        s = r_.sc[c % 2, k * R + at : k * R + at + STRIP] + r_.bias[at : at + STRIP, rows]
                        top = jnp.max(s, 1, keepdims=True)
                        e = jnp.exp2((s - top) * factor_exp)
                        r_.tp[2 * c + k, at : at + STRIP] = jnp.broadcast_to(top, (STRIP, 128))
                        first = (hf * HK + 2 * c + k) * R + at
                        r_.pst[l, first : first + STRIP, rows] = e.astype(BF16)
                for k in range(2):
                    h = 2 * c + k
                    left = jnp.concatenate([r_.kvT[l, head_dims(hf, h, D), rows], ones], 0)
                    o = dot_nt(left, r_.pst[l, head_rows(hf, h), rows])
                    r_.odT[i, head_dims(hf, h)] = o[0:HEAD_DIM]
                    r_.ldT[i, head_dims(hf, h)] = o[HEAD_DIM:]
            r_.md[i, :, lanes] = by_head([r_.tp[k] for k in range(HK)])

    def attention_end(l):
        tops = [r_.md[i].T for i in range(NB)]
        top = tops[0]
        for i in range(1, NB):
            top = jnp.maximum(top, tops[i])
        factors = [jnp.exp2((tops[i] - top) * factor_exp) for i in range(NB)]
        inv = 1.0 / sum(factors[i] * r_.ldT[i] for i in range(NB))
        o = jnp.zeros((D, R), F32)
        for i in range(NB):
            r_.rb[l, i] = (factors[i] * inv).T
            o = o + factors[i] * inv * r_.odT[i]
        o = o.T
        r_.oraw[l] = o
        ob = o.astype(BF16)
        r_.ob[l] = ob
        t1 = r_.xf[l] + dot(ob, r_.wo[l])
        r_.z1[l] = t1
        mean1 = col_sum(t1) / R
        return mean1, col_sum((t1 - mean1) * (t1 - mean1))

    def convolution(l):
        xs = r_.xs
        xb = xs[l, me]
        r_.xe[l, 0:R] = xb
        arrive(r_.xe.at[l, R : R + 64], r_.hx_r.at[l])
        xe = r_.xe[l]
        made = dot(xe, r_.wp[l])
        pd_high, pd_low = split(made[:, 2 * D : 3 * D])
        r_.re[0:256] = made[:, 3 * D :].astype(BF16)
        r_.re[256:512] = r_.we[l]
        r_.re[512:768] = pd_high
        r_.re[768:1024] = pd_low
        r_.gate[l] = dot(r_.le[...], r_.re[...])
        r_.bs[l] = dot(r_.le[:, 0:256], made[:, D : 2 * D].astype(BF16)).astype(BF16)
        for at in range(0, E, 64):
            here = slice(at, at + 64)
            gate = sigmoid(r_.gate[l, here])
            r_.gate[l, here] = gate
            high, low = split(jnp.concatenate([gate * r_.bs[l, here].astype(F32), gate], 1))
            r_.gg[here] = high
            r_.gg[E + at : E + at + 64] = low
        num_den = dot(r_.TT[...], r_.gg[...])
        pa, num, den = made[0:R, 0:D], num_den[:, 0:D], num_den[:, D:]
        r_.num[l] = num
        r_.den[l] = den
        msg = pa + num / (den + GATE_EPS)
        r_.z0[l] = msg
        mean0 = col_sum(msg) / R
        return mean0, col_sum((msg - mean0) * (msg - mean0))

    def forward(l):
        def ready(js):
            for j in js:
                moved = (r_.gb[l, j].astype(F32) + r_.moff[j, 0:1]) * r_.move[0:1] + r_.move[1:2]
                r_.xs[l, j] = moved.astype(BF16)

        r_.xs[l, me] = r_.xf[l].astype(BF16)
        r_.hx[l] = dot(r_.HS[...], r_.xs[l, me]).astype(BF16)
        send(r_.hx.at[l, 0:32], r_.xe.at[l, R + 32 : R + 64], r_.hx_s.at[0], r_.hx_r.at[l], nodes=prev)
        send(r_.hx.at[l, 32:64], r_.xe.at[l, R : R + 32], r_.hx_s.at[0], r_.hx_r.at[l], nodes=nxt)
        prepare_queries(l)
        for t in range(2, NZ):
            gather_pass(l, t)
        mean0, sq0 = convolution(l)
        sync_start(3 * l, mean0, sq0)
        gather_near(l)
        ready([partner, 2 * z_from(1) + par, 2 * z_from(1) + 1 - par])

        attention_keys(l, 0)
        attention_heads(l, 0, (0, 1))
        gather_far(l)
        ready([2 * z_from(t) + p for t in range(2, NZ) for p in range(2)])
        for i in range(1, NB):
            attention_keys(l, i)
            attention_heads(l, i, (0, 1))
        mean1, sq1 = attention_end(l)
        sync_start(3 * l + 1, mean1, sq1)
        mean0, sq0 = sync_moments(3 * l)
        inv0 = lax.rsqrt(sq0 / total + NORM_EPS)
        r_.iv[l, 0:1] = inv0
        z0 = (r_.z0[l] - mean0) * inv0
        r_.z0[l] = z0
        n0 = z0 * r_.gain[l, 0:1] + r_.shift[l, 0:1]
        r_.local[...] = r_.xf[l] + n0 * sigmoid(n0)
        mean1, sq1 = sync_moments(3 * l + 1)
        inv1 = lax.rsqrt(sq1 / total + NORM_EPS)
        r_.iv[l, 1:2] = inv1
        z1 = (r_.z1[l] - mean1) * inv1
        r_.z1[l] = z1
        mix = r_.local[...] + z1 * r_.gain[l, 1:2] + r_.shift[l, 1:2]
        mb = mix.astype(BF16)
        r_.mb[l] = mb
        u = dot(mb, r_.wu[l])
        r_.u[l] = u
        g = (u * sigmoid(u)).astype(BF16)
        r_.g[l] = g
        y = mix + dot(g, r_.wd[l])
        r_.z2[l] = y
        mean = col_sum(y) / R
        cent = y - mean
        k = 3 * l + 2
        sync_start(k, mean, col_sum(cent * cent))

        if l < L - 1:
            r_.gb[l + 1, me] = cent.astype(BF16)
            gather_start(l + 1)

        if l == L - 1:
            dy = r_.cot[...].astype(F32)
            sync_start(3 * L, col_sum(dy), col_sum(dy * cent))

        tot_mean, tot_sq = sync_moments(k)
        inv2 = lax.rsqrt(tot_sq / total + NORM_EPS)
        r_.iv[l, 2:3] = inv2
        z2 = (r_.z2[l] - tot_mean) * inv2
        r_.z2[l] = z2
        gain, shift = r_.gain[l, 2:3], r_.shift[l, 2:3]
        r_.xf[l + 1] = z2 * gain + shift

        if l == L - 1:
            sync_wait(3 * L)
            sums, means = r_.st1[3 * L], r_.st1[k][:, 0:2]
            mean = jnp.mean(means, 0)
            dy_sum = jnp.sum(sums[:, 0:2], 0)
            dy_cent = jnp.sum(sums[:, 2:4] + (means - mean) * sums[:, 0:2], 0)
            dy_sum, dy_cent = unpack(jnp.concatenate([dy_sum, dy_cent], 0))
            r_.gshift[l, 2:3] = dy_sum
            r_.ggain[l, 2:3] = dy_cent * inv2

        for j in range(N):
            tile = r_.st1[k, rep * N + j]
            r_.moff[j, 0:1] = jnp.concatenate([tile[0:1], tile[1:2]], 1) - tot_mean
        r_.move[0:1] = inv2 * gain
        r_.move[1:2] = shift

    for l in range(L):
        forward(l)
    act_copy = pltpu.make_async_copy(r_.xf.at[L], r_.out_act, r_.store.at[0])
    act_copy.start()

    def back_feed_forward(l, k):
        s2, g2 = r_.gshift[l, 2:3], r_.ggain[l, 2:3]
        d3 = r_.gain[l, 2:3] * r_.iv[l, 2:3] * (r_.dy[...] - s2 / total - r_.z2[l] * (g2 / total))
        db = d3.astype(BF16)
        dub = (dot_nt(db, r_.wd[l]) * silu_slope(r_.u[l])).astype(BF16)
        dmix = d3 + dot_nt(dub, r_.wu[l])
        r_.dmix[...] = dmix
        n0 = r_.z0[l] * r_.gain[l, 0:1] + r_.shift[l, 0:1]
        gy0 = dmix * silu_slope(n0)
        sync_start(k, col_sum(dmix), col_sum(dmix * r_.z1[l]))
        sync_start(k + 1, col_sum(gy0), col_sum(gy0 * r_.z0[l]))
        r_.gy0[...] = gy0
        at = put(r_.gs_early, l, 512, dot_tn(r_.mb[l], dub))
        put(r_.gs_early, l, at, dot_tn(r_.g[l], db))
        r_.xeT[...] = r_.xe[l].T
        r_.qT[...] = r_.q[l].T

    def back_norms(l, k):
        s1, g1 = sync_sums(k)
        r_.gshift[l, 1:2] = s1
        r_.ggain[l, 1:2] = g1
        dmix = r_.dmix[...]
        d2 = r_.gain[l, 1:2] * r_.iv[l, 1:2] * (dmix - s1 / total - r_.z1[l] * (g1 / total))
        dab = d2.astype(BF16)
        r_.dxo[...] = dmix + d2
        r_.dob[...] = dot_nt(dab, r_.wo[l]).astype(BF16).astype(F32)
        put(r_.gs_early, l, 0, dot_tn(r_.ob[l], dab))
        r_.gkv[...] = jnp.zeros((2 * D, D), F32)
        r_.dqT[...] = jnp.zeros((D, R), F32)

    def back_half(i):
        t1 = (i + 1) % NB
        half = (zh + t1) % NB
        place = (NB - t1) % NB
        return place, half, slice(place * W, (place + 1) * W)

    def back_heads(l, i, hf):
        place, half, rows = back_half(i)
        if True:
            lanes = lane_half(hf)
            dos = r_.dob[:, lanes] * r_.rb[l, place, :, lanes]
            prod = dos * r_.oraw[l, :, lanes]
            for k in range(HK):
                r_.dom[k * R : (k + 1) * R, 0:128] = jnp.where(lane_head == k, dos, 0.0).astype(BF16)
                r_.dom[k * R : (k + 1) * R, 128:256] = jnp.where(lane_head == k, -prod, 0.0).astype(BF16)
            r_.dosT[...] = dos.T.astype(BF16)
            values = slice(D + hf * 128, D + (hf + 1) * 128)
            right = jnp.concatenate([r_.kvT[l, values, rows], jnp.ones((128, W), BF16)], 0)
            for c in range(HK // 2):
                both = slice(2 * c * R, 2 * (c + 1) * R)
                r_.sc[c % 2, 0 : 2 * R] = dot(r_.dom[both], right)
                for k in range(2):
                    for at in range(0, R, STRIP):
                        first = (hf * HK + 2 * c + k) * R + at
                        e = r_.pst[l, first : first + STRIP, rows].astype(F32)
                        ds = e * r_.sc[c % 2, k * R + at : k * R + at + STRIP]
                        r_.dss[(2 * c + k) * R + at : (2 * c + k) * R + at + STRIP] = ds.astype(BF16)
                for k in range(2):
                    h = 2 * c + k
                    mine, dims = slice(h * R, (h + 1) * R), head_dims(hf, h)
                    r_.dqT[dims] += dot_nt(r_.kvT[l, dims, rows], r_.dss[mine])
                    r_.dkv[dims] = (dot(r_.qT[dims], r_.dss[mine]) * scale).astype(BF16)
                    dv = dot(r_.dosT[h * HEAD_DIM : (h + 1) * HEAD_DIM], r_.pst[l, head_rows(hf, h), rows])
                    r_.dkv[head_dims(hf, h, D)] = dv.astype(BF16)

    def back_rows(l, i):
        _, half, _ = back_half(i)
        dx = dot(r_.wqkv[l, :, D:], r_.dkv[...]).T
        r_.dxs[l, pl.ds(2 * half, 2)] = dx.astype(BF16).reshape(2, 2, R, D)

        if i < NB - 1:
            for t in (2 * (i + 1), 2 * (i + 1) + 1):
                zb = z_to(t)
                send_rows(r_.dxs.at[l, zb, 1 - par], r_.rs1.at[l, zb], R,
                          r_.rs_s.at[0], r_.rsp_r.at[l, i, t % 2], nodes=partner)

        else:
            near = z_to(1)
            send_rows(r_.dxs.at[l, z, 1 - par], r_.ro.at[l, 0], R, r_.rs_s.at[0], r_.ro_r.at[l], nodes=partner)
            send_rows(r_.dxs.at[l, near, par], r_.ro.at[l, 1], R, r_.rs_s.at[0], r_.ro_r.at[l], nodes=2 * near + par)
            send_rows(r_.dxs.at[l, near, 1 - par], r_.ro.at[l, 2], R, r_.rs_s.at[0], r_.ro_r.at[l],
                 nodes=2 * near + 1 - par)

        r_.gkv[...] += dot(r_.dkv[...], r_.xs[l, pl.ds(4 * half, 4)].reshape(W, D))

    def pass_on(l, i, t):
        zb = z_to(t)
        arrive(r_.rs1.at[l, zb], r_.rsp_r.at[l, i, t % 2])
        both = r_.dxs[l, zb, par].astype(F32) + r_.rs1[l, zb].astype(F32)
        r_.cs[l, zb] = both.astype(BF16)
        send_rows(r_.cs.at[l, zb], r_.rs2.at[l, z], R, r_.rs_s.at[0], r_.rsc_r.at[l], nodes=2 * zb + par)

    def back_convolution(l, k):
        s0, g0 = unpack(jnp.sum(r_.st1[k + 1], 0))
        r_.gshift[l, 0:1] = s0
        r_.ggain[l, 0:1] = g0
        inv_den = 1.0 / (r_.den[l] + GATE_EPS)
        dm = r_.gain[l, 0:1] * r_.iv[l, 0:1] * (r_.gy0[...] - s0 / total - r_.z0[l] * (g0 / total))
        dnum = dm * inv_den
        dden = -dnum * r_.num[l] * inv_den
        high, low = split(jnp.concatenate([dnum, dden], 1))
        r_.dn[0:R] = high
        r_.dn[256 : 256 + R] = low
        r_.sc[0, 0:E, 0 : 2 * D] = dot(r_.le[:, 512:1024], r_.dn[...])
        for at in range(0, E, 64):
            here = slice(at, at + 64)
            gate, dnum_e = r_.gate[l, here], r_.sc[0, here, 0:D]
            dgp = (dnum_e * r_.bs[l, here].astype(F32) + r_.sc[0, here, D : 2 * D]) * gate * (1.0 - gate)
            r_.gg[here, 0:D] = (dnum_e * gate).astype(BF16)
            r_.gg[here, D:] = dgp.astype(BF16)
        ext = dot(r_.ST[...], r_.gg[0:E]).astype(BF16)
        r_.dproj[0:R, 0:D] = dm.astype(BF16)
        r_.dproj[:, D : 2 * D] = ext[:, 0:D]
        r_.dproj[0:R, 2 * D : 3 * D] = dot(r_.TT[:, 0:E], r_.gg[0:E, D:]).astype(BF16)
        r_.dproj[:, 3 * D :] = ext[:, D:]
        dxe = dot_nt(r_.dproj[...], r_.wp[l])
        r_.hs[l, 0] = dxe[R : R + 32].astype(BF16)
        r_.hs[l, 1] = dxe[R + 32 : R + 64].astype(BF16)
        r_.dxo[...] += dxe[0:R]

    def send_halo(l):
        send(r_.hs.at[l, 0], r_.hr.at[l, 1], r_.hal_s.at[0], r_.hal_r.at[l], nodes=prev)
        send(r_.hs.at[l, 1], r_.hr.at[l, 0], r_.hal_s.at[0], r_.hal_r.at[l], nodes=nxt)

    def conv_weight_grads(l):
        at = put(r_.gs_conv, l, 0, dot(r_.xeT[...], r_.dproj[...]))
        put(r_.gs_conv, l, at, dot(r_.efT[...], r_.gg[0:E, D:]))

    def back_input(l):
        dx = r_.dxo[...]
        dx = dx + r_.dxs[l, z, par].astype(F32)
        arrive(r_.ro.at[l], r_.ro_r.at[l])
        for slot in range(3):
            dx = dx + r_.ro[l, slot].astype(F32)
        if NZ > 2:
            arrive(r_.rs2.at[l, 0 : NZ - 2], r_.rsc_r.at[l])
        for t in range(2, NZ):
            dx = dx + r_.rs2[l, z_from(t)].astype(F32)
        arrive(r_.hr.at[l], r_.hal_r.at[l])
        back = jnp.concatenate(
            [r_.hr[l, 0].astype(F32)[0:24], r_.hr[l, 1].astype(F32)[0:24], jnp.zeros((16, D), F32)], 0
        )
        return dx + dot(r_.A[...], back.astype(BF16))

    r_.dy[...] = r_.cot[...].astype(F32)

    E1, C1, Q1, E0, C0, QK0, V0 = range(len(GROUPS))

    def steps(*pairs):
        return [functools.partial(reduce_step, g, k) for g, k in pairs]

    r_.dy[...] = r_.cot[...].astype(F32)

    def backward(b):
        l = L - 1 - b
        first, last = b == 0, b == L - 1
        k = 3 * L + 1 + 2 * b
        back_feed_forward(l, k)
        when(last, *steps((E1, 3), (C1, 3), (Q1, 2)))
        back_norms(l, k)
        if first:
            when(True, *steps((E1, 0)))
            back_heads(l, 0, 0)
            back_heads(l, 0, 1)
            back_rows(l, 0)
            when(True, *steps((E1, 1)))
            sync_wait(k + 1)
            back_convolution(l, k)
            send_halo(l)
            pass_on(l, 0, 2)
            back_heads(l, 1, 0)
            pass_on(l, 0, 3)
            back_heads(l, 1, 1)
            back_rows(l, 1)
            conv_weight_grads(l)
            when(True, *steps((C1, 0)))
        else:
            when(True, *steps((E1, 4), (C1, 4), (Q1, 3), (E0, 0)))
            sync_wait(k + 1)
            back_convolution(l, k)
            send_halo(l)
            conv_weight_grads(l)
            when(True, *steps((E0, 1), (C0, 0)))
            back_heads(l, 0, 0)
            when(True, *steps((E1, 5), (C1, 5), (Q1, 4), (C0, 1)))
            back_heads(l, 0, 1)
            back_rows(l, 0)
            when(True, *steps((E0, 2), (E1, 6), (C1, 6), (Q1, 5)))
            back_heads(l, 1, 0)
            when(True, *steps((E0, 3), (C0, 2), (E1, 7), (C1, 7), (Q1, 6)))
            for t in range(2, NZ):
                pass_on(l, 0, t)
            back_heads(l, 1, 1)
            back_rows(l, 1)
            when(True, *steps((E0, 4), (C0, 3), (E1, 8), (C1, 8), (Q1, 7)))
        dqb = (r_.dqT[...].T * scale).astype(BF16)
        r_.dxo[...] += dot_nt(dqb, r_.wqkv[l, :, 0:D])
        at = put(r_.gs_qkv, l, 0, dot(r_.xeT[:, 0:R], dqb))
        put(r_.gs_qkv, l, at, r_.gkv[...].T)
        if first:
            when(True, *steps((Q1, 0), (C1, 1)))
            dx = back_input(l)
            r_.dy[...] = dx
            below = L - 2
            sync_start(SYNCS - 1, col_sum(dx), col_sum(dx * r_.z2[below]))
            when(True, *steps((E1, 2), (Q1, 1)))
            s2, g2 = sync_sums(SYNCS - 1)
            r_.gshift[below, 2:3] = s2
            r_.ggain[below, 2:3] = g2
            when(True, *steps((C1, 2)))

    for b in range(L):
        backward(b)
    for step in steps((QK0, 0), (V0, 0), (E0, 5), (C0, 4), (V0, 1), (QK0, 1), (Q1, 8)):
        step()
    r_.dy[...] = back_input(0)
    in_copy = pltpu.make_async_copy(r_.dy, r_.grad_in, r_.store.at[1])
    in_copy.start()
    for step in steps(
        (E0, 6), (C0, 5), (V0, 2), (QK0, 2),
        (E0, 7), (C0, 6), (V0, 3), (QK0, 3),
        (E0, 8), (C0, 7), (V0, 4), (QK0, 4), (C0, 8),
    ):
        step()
    for l in range(L):
        for k in range(3):
            r_.ggain_out[k, l : l + 1] = r_.ggain[l, k : k + 1]
            r_.gshift_out[k, l : l + 1] = r_.gshift[l, k : k + 1]
    for g in range(len(GROUPS)):
        reduce_drain(g)
    sent(r_.meta.at[0 : N - 1], r_.meta_s.at[0])
    sent(r_.st1.at[:, 0 : M * N - 1], r_.st_s.at[0])
    sent(r_.gb.at[:, 0 : 3 + 2 * (NZ - 2)], r_.ag_s.at[0])
    sent(r_.gb.at[:, 0 : 2 * (NB - 1) + 3 + NZ - 2], r_.rs_s.at[0])
    sent(r_.hs, r_.hal_s.at[0])
    sent(r_.hx, r_.hx_s.at[0])
    act_copy.wait()
    in_copy.wait()


def finish_kernel(act_h, gin_h, *refs):
    n = len(GROUPS)
    held, (ggain_h, gshift_h), refs = refs[:n], refs[n : n + 2], refs[n + 2 :]
    act_o, gin_o, proj_o, edge_o, qkv_o, out_o, up_o, down_o, ggain_o, gshift_o = refs[:10]
    summed, refs = refs[10 : 10 + n], refs[10 + n :]
    act, gin, proj, edge, qkv, out, up, down, in_sem, out_sem = refs
    loads = [
        pltpu.make_async_copy(src, dst, in_sem.at[i])
        for i, (src, dst) in enumerate(zip(held + (act_h, gin_h), summed + (act, gin), strict=True))
    ]
    for load in loads:
        load.start()
    ggain_o[...] = ggain_h[...]
    gshift_o[...] = gshift_h[...]
    stores = []

    def store(src, dst):
        copy = pltpu.make_async_copy(src, dst, out_sem.at[len(stores)])
        copy.start()
        stores.append(copy)

    def widen(dst, l, g, at, first=0, last=None):
        rows = dst.shape[1]
        for c in range(first, dst.shape[2] // 128 if last is None else last):
            dst[l, :, 128 * c : 128 * (c + 1)] = summed[g][at : at + rows].astype(F32)
            at += rows
        return at

    for g, (name, l, first, rows, _) in enumerate(GROUPS):
        loads[g].wait()
        if name == "early":
            at = widen(out, l, g, 0)
            store(out.at[l], out_o.at[l])
            at = widen(up, l, g, at)
            store(up.at[l], up_o.at[l])
            widen(down, l, g, at)
            store(down.at[l], down_o.at[l])
        elif name == "conv":
            at = widen(proj, l, g, 0)
            store(proj.at[l], proj_o.at[l])
            widen(edge, l, g, at)
            store(edge.at[l], edge_o.at[l])
        else:
            widen(qkv, l, g, 0, first // 256, (first + rows) // 256)
            if first + rows == 1536:
                store(qkv.at[l], qkv_o.at[l])
    for i, (src, dst) in enumerate(((act, act_o), (gin, gin_o))):
        loads[n + i].wait()
        store(src, dst)
    for copy in stores:
        copy.wait()


def fused_device(
    N, M, node_input, edge_feat, graph_ids, edge_src, edge_dst, halo_send, w_proj, w_edge, w_qkv,
    w_out, w_up, w_down, norm_gain, norm_shift, cotangent,
):
    R, D = node_input.shape
    E = edge_feat.shape[0]
    L = w_proj.shape[0]
    names = scratch_list(N, M, L, R, E)
    vmem = pl.BlockSpec(memory_space=pltpu.VMEM)
    hbm = pl.BlockSpec(memory_space=pltpu.HBM)
    shape = jax.ShapeDtypeStruct
    rows = shape((R, D), F32)
    norm = shape((3, L, D), F32)
    groups = [shape((rows_g, 128), BF16) for _, _, _, rows_g, _ in GROUPS]
    outs = pl.pallas_call(
        functools.partial(kernel, N, M, L, tuple(names)),
        out_shape=[rows, rows, *groups, norm, norm],
        in_specs=[hbm] + [vmem] * 4 + [hbm] * 7 + [vmem] * 2 + [hbm],
        out_specs=[hbm] * (2 + len(GROUPS)) + [vmem] * 2,
        scratch_shapes=list(names.values()),
        compiler_params=pltpu.CompilerParams(
            collective_id=0, has_side_effects=True, vmem_limit_bytes=60 << 20
        ),
        name="layers",
    )(node_input, graph_ids, edge_src, edge_dst, halo_send, edge_feat, w_proj, w_edge, w_qkv, w_out, w_up,
      w_down, norm_gain.transpose(1, 0, 2), norm_shift.transpose(1, 0, 2), cotangent)
    weights = [shape(w.shape, F32) for w in (w_proj, w_edge, w_qkv, w_out, w_up, w_down)]
    results = pl.pallas_call(
        finish_kernel,
        out_shape=[rows, rows, *weights, norm, norm],
        in_specs=[hbm] * (2 + len(GROUPS)) + [vmem] * 2,
        out_specs=[hbm] * 8 + [vmem] * 2,
        scratch_shapes=[pltpu.VMEM(s.shape, s.dtype) for s in (*groups, rows, rows, *weights)]
        + [pltpu.SemaphoreType.DMA((len(GROUPS) + 2,)), pltpu.SemaphoreType.DMA((14,))],
        compiler_params=pltpu.CompilerParams(vmem_limit_bytes=60 << 20),
        name="gradients",
    )(*outs)
    ggain, gshift = results[8].transpose(1, 0, 2), results[9].transpose(1, 0, 2)
    return (*results[:8], ggain, gshift)


BLOCK_CAP = 2048


def extended_2(block, sides, width):
    for axis, dim in sides:
        count = lax.axis_size(axis)
        forward = [(i, i + 1) for i in range(count - 1)]
        forward.append((count - 1, 0))
        backward = [(target, source) for source, target in forward]
        low = lax.ppermute(
            lax.slice_in_dim(block, block.shape[dim] - width, None, axis=dim), axis, forward
        )
        high = lax.ppermute(lax.slice_in_dim(block, 0, width, axis=dim), axis, backward)
        block = jnp.concatenate([low, block, high], axis=dim)
    return block


def block_length(total_rows, upper_limit):
    for length in range(min(total_rows, upper_limit), 0, -1):
        if total_rows % length == 0:
            return length
    return 1


def outer_product(left, right):
    return lax.dot_general(
        left, right, (((0,), (0,)), ((), ())), preferred_element_type=jnp.float32
    )


def times_transposed(left, weight):
    return lax.dot_general(
        left, weight, (((1,), (1,)), ((), ())), preferred_element_type=jnp.float32
    )


def forward_product(left, weight):
    return jnp.dot(left, weight, preferred_element_type=jnp.float32)


def silu_slope_plain(inputs):
    logistic = jax.nn.sigmoid(inputs)
    return logistic * (1.0 + inputs * (1.0 - logistic))


def normalize(inputs, gain_row, shift_row, node_total):
    batch_mean = lax.psum(jnp.sum(inputs, 0), ("nodes", "rep")) / node_total
    centred = inputs - batch_mean
    batch_var = lax.psum(jnp.sum(centred * centred, 0), ("nodes", "rep")) / node_total
    inv_std = lax.rsqrt(batch_var + NORM_EPS)
    standard = (inputs - batch_mean) * inv_std
    return (standard * gain_row + shift_row, standard, inv_std)


def normalize_back(grad_out, standard, inv_std, gain_row, node_total):
    shift_grad, gain_grad = lax.psum(
        (jnp.sum(grad_out, 0), jnp.sum(grad_out * standard, 0)), ("nodes", "rep")
    )
    grad_in = (
        gain_row
        * inv_std
        * (grad_out - shift_grad / node_total - standard * gain_grad / node_total)
    )
    return (grad_in, gain_grad, shift_grad)


def exchange_sources(outgoing):
    halo_rows = outgoing.shape[0] // 2
    grown = extended_2(outgoing, (("nodes", 0),), halo_rows)
    return jnp.concatenate([grown[:halo_rows], grown[3 * halo_rows :]], 0)


def return_sources(incoming_grad):
    halo_rows = incoming_grad.shape[0] // 2
    grown = extended_2(incoming_grad.astype(jnp.bfloat16), (("nodes", 0),), halo_rows).astype(
        incoming_grad.dtype
    )
    return jnp.concatenate([grown[:halo_rows], grown[3 * halo_rows :]], 0)


def attend_forward(query_rows, key_rows, value_rows, local_graphs, group_graphs):
    row_count = query_rows.shape[0]
    score_scale = HEAD_DIM ** (-0.5)
    queries = query_rows.reshape(row_count, HEADS, HEAD_DIM)

    def add_piece(carried, kv_piece, first_row):
        key_piece, value_piece = kv_piece
        piece_rows = key_piece.shape[0]
        block_len = block_length(piece_rows, BLOCK_CAP)

        def add_block(block_state, block_index):
            row_max, row_sum, accumulated = block_state
            block_start = block_index * block_len
            key_block = lax.dynamic_slice_in_dim(key_piece, block_start, block_len, 0).reshape(
                block_len, HEADS, HEAD_DIM
            )
            value_block = lax.dynamic_slice_in_dim(value_piece, block_start, block_len, 0).reshape(
                block_len, HEADS, HEAD_DIM
            )
            key_graphs = lax.dynamic_slice_in_dim(
                group_graphs, first_row + block_start, block_len, 0
            )
            same_graph = (local_graphs[:, None] == key_graphs[None, :])[None]
            scores = (
                jnp.einsum("qhd,khd->hqk", queries, key_block, preferred_element_type=jnp.float32)
                * score_scale
            )
            scores = jnp.where(same_graph, scores, NEG)
            new_max = jnp.maximum(row_max, jnp.max(scores, 2))
            weights = jnp.where(same_graph, jnp.exp(scores - new_max[:, :, None]), 0.0)
            factor = jnp.exp(row_max - new_max)
            row_sum = row_sum * factor + jnp.sum(weights, 2)
            contrib = jnp.einsum(
                "hqk,khd->qhd",
                weights.astype(jnp.bfloat16),
                value_block,
                preferred_element_type=jnp.float32,
            )
            accumulated = accumulated * jnp.transpose(factor)[:, :, None] + contrib
            return ((new_max, row_sum, accumulated), None)

        carried, _ = lax.scan(add_block, carried, jnp.arange(piece_rows // block_len))
        return carried

    start_state = (
        jnp.full((HEADS, row_count), NEG, jnp.float32),
        jnp.zeros((HEADS, row_count), jnp.float32),
        jnp.zeros((row_count, HEADS, HEAD_DIM), jnp.float32),
    )
    row_max, row_sum, accumulated = add_piece(
        start_state,
        (
            lax.all_gather(key_rows, "nodes", axis=0, tiled=True),
            lax.all_gather(value_rows, "nodes", axis=0, tiled=True),
        ),
        jnp.int32(0),
    )
    attn_raw = accumulated / jnp.transpose(row_sum)[:, :, None]
    log_sum = row_max + jnp.log(row_sum)
    return (attn_raw, log_sum)


def attend_backward(
    query_rows, key_rows, value_rows, grad_low, attn_raw, log_sum, local_graphs, group_graphs
):
    row_count = query_rows.shape[0]
    model_width = HEADS * HEAD_DIM
    score_scale = HEAD_DIM ** (-0.5)
    queries = query_rows.reshape(row_count, HEADS, HEAD_DIM)
    grad_heads = grad_low.reshape(row_count, HEADS, HEAD_DIM)
    row_delta = jnp.einsum("qhd,qhd->hq", grad_heads.astype(jnp.float32), attn_raw)

    def score_block(key_block, value_block, key_graphs):
        same_graph = (local_graphs[:, None] == key_graphs[None, :])[None]
        scores = (
            jnp.einsum("qhd,khd->hqk", queries, key_block, preferred_element_type=jnp.float32)
            * score_scale
        )
        attn_weights = jnp.exp(jnp.where(same_graph, scores - log_sum[:, :, None], NEG))
        grad_weights = jnp.einsum(
            "qhd,khd->hqk", grad_heads, value_block, preferred_element_type=jnp.float32
        )
        grad_scores = (attn_weights * (grad_weights - row_delta[:, :, None])).astype(jnp.bfloat16)
        return (attn_weights, grad_scores)

    def key_terms(attn_weights, grad_scores, block_len):
        grad_keys = (
            jnp.einsum("hqk,qhd->khd", grad_scores, queries, preferred_element_type=jnp.float32)
            * score_scale
        )
        grad_values = jnp.einsum(
            "hqk,qhd->khd",
            attn_weights.astype(jnp.bfloat16),
            grad_heads,
            preferred_element_type=jnp.float32,
        )
        return jnp.concatenate(
            [
                grad_keys.reshape(block_len, model_width),
                grad_values.reshape(block_len, model_width),
            ],
            1,
        )

    def query_term(grad_scores, key_block):
        return (
            jnp.einsum("hqk,khd->qhd", grad_scores, key_block, preferred_element_type=jnp.float32)
            * score_scale
        )

    group_rows = group_graphs.shape[0]

    def add_piece(carried, kv_piece, first_row):
        key_piece, value_piece = kv_piece
        piece_rows = key_piece.shape[0]
        block_len = block_length(piece_rows, BLOCK_CAP)

        def add_block(block_state, block_index):
            grad_query, buffer = block_state
            block_start = block_index * block_len
            key_block = lax.dynamic_slice_in_dim(key_piece, block_start, block_len, 0).reshape(
                block_len, HEADS, HEAD_DIM
            )
            value_block = lax.dynamic_slice_in_dim(value_piece, block_start, block_len, 0).reshape(
                block_len, HEADS, HEAD_DIM
            )
            place = first_row + block_start
            key_graphs = lax.dynamic_slice_in_dim(group_graphs, place, block_len, 0)
            attn_weights, grad_scores = score_block(key_block, value_block, key_graphs)
            grad_query = grad_query + query_term(grad_scores, key_block)
            block_terms = key_terms(attn_weights, grad_scores, block_len)
            current = lax.dynamic_slice_in_dim(buffer, place, block_len, 0)
            buffer = lax.dynamic_update_slice_in_dim(buffer, current + block_terms, place, 0)
            return ((grad_query, buffer), None)

        carried, _ = lax.scan(add_block, carried, jnp.arange(piece_rows // block_len))
        return carried

    start_state = (
        jnp.zeros((row_count, HEADS, HEAD_DIM), jnp.float32),
        jnp.zeros((group_rows, 2 * model_width), jnp.float32),
    )
    grad_query, buffer = add_piece(
        start_state,
        (
            lax.all_gather(key_rows, "nodes", axis=0, tiled=True),
            lax.all_gather(value_rows, "nodes", axis=0, tiled=True),
        ),
        jnp.int32(0),
    )
    grad_kv = lax.psum_scatter(buffer, "nodes", scatter_dimension=0, tiled=True)
    return (
        grad_query.reshape(row_count, model_width),
        grad_kv[:, :model_width],
        grad_kv[:, model_width:],
    )


def layer_forward(
    hidden, params, edge_feat, edge_src, edge_dst, halo_send, local_graphs, group_graphs, node_total
):
    w_proj, w_edge, w_qkv, w_out, w_up, w_down, norm_gains, norm_shifts = params
    row_count, model_width = hidden.shape
    hidden_low = hidden.astype(jnp.bfloat16)
    projected = forward_product(hidden_low, w_proj)
    self_term = projected[:, :model_width]
    dest_term = projected[:, 2 * model_width : 3 * model_width]
    source_rows = jnp.concatenate(
        [projected[:, model_width : 2 * model_width], projected[:, 3 * model_width :]], 1
    ).astype(jnp.bfloat16)
    incoming = exchange_sources(source_rows[halo_send])
    extended = jnp.concatenate([source_rows, incoming], 0)
    edge_rows = extended[edge_src].astype(jnp.float32)
    source_b = edge_rows[:, :model_width]
    source_e = edge_rows[:, model_width:]
    edge_proj = forward_product(edge_feat, w_edge)
    gating = jax.nn.sigmoid(dest_term[edge_dst] + source_e + edge_proj)
    numerator = jax.ops.segment_sum(gating * source_b, edge_dst, row_count)
    denominator = jax.ops.segment_sum(gating, edge_dst, row_count)
    message = self_term + numerator / (denominator + GATE_EPS)
    normed_one, standard_one, inv_one = normalize(
        message, norm_gains[0], norm_shifts[0], node_total
    )
    local_out = hidden + jax.nn.silu(normed_one)
    qkv_low = forward_product(hidden_low, w_qkv).astype(jnp.bfloat16)
    query_rows = qkv_low[:, :model_width]
    key_rows = qkv_low[:, model_width : 2 * model_width]
    value_rows = qkv_low[:, 2 * model_width :]
    attn_raw, log_sum = attend_forward(query_rows, key_rows, value_rows, local_graphs, group_graphs)
    attn_low = attn_raw.reshape(row_count, model_width).astype(jnp.bfloat16)
    attn_proj = forward_product(attn_low, w_out)
    normed_two, standard_two, inv_two = normalize(
        hidden + attn_proj, norm_gains[1], norm_shifts[1], node_total
    )
    mixed = local_out + normed_two
    mixed_low = mixed.astype(jnp.bfloat16)
    up_proj = forward_product(mixed_low, w_up)
    activated = jax.nn.silu(up_proj).astype(jnp.bfloat16)
    down_proj = forward_product(activated, w_down)
    normed_three, standard_three, inv_three = normalize(
        mixed + down_proj, norm_gains[2], norm_shifts[2], node_total
    )
    saved = (
        hidden_low,
        source_b,
        gating,
        numerator,
        denominator,
        normed_one,
        standard_one,
        inv_one,
        query_rows,
        key_rows,
        value_rows,
        attn_raw,
        log_sum,
        attn_low,
        standard_two,
        inv_two,
        mixed_low,
        up_proj,
        activated,
        standard_three,
        inv_three,
    )
    return (normed_three, saved)


def layer_backward(
    grad_out,
    params,
    saved,
    edge_feat,
    edge_src,
    edge_dst,
    halo_send,
    local_graphs,
    group_graphs,
    node_total,
):
    w_proj, w_edge, w_qkv, w_out, w_up, w_down, norm_gains, norm_shifts = params
    (
        hidden_low,
        source_b,
        gating,
        numerator,
        denominator,
        normed_one,
        standard_one,
        inv_one,
        query_rows,
        key_rows,
        value_rows,
        attn_raw,
        log_sum,
        attn_low,
        standard_two,
        inv_two,
        mixed_low,
        up_proj,
        activated,
        standard_three,
        inv_three,
    ) = saved
    row_count, model_width = grad_out.shape
    grad_three, gain_three, shift_three = normalize_back(
        grad_out, standard_three, inv_three, norm_gains[2], node_total
    )
    down_grad = grad_three.astype(jnp.bfloat16)
    grad_w_down = outer_product(activated, down_grad)
    up_grad = (times_transposed(down_grad, w_down) * silu_slope_plain(up_proj)).astype(jnp.bfloat16)
    grad_w_up = outer_product(mixed_low, up_grad)
    grad_mixed = grad_three + times_transposed(up_grad, w_up)
    grad_two, gain_two, shift_two = normalize_back(
        grad_mixed, standard_two, inv_two, norm_gains[1], node_total
    )
    out_grad = grad_two.astype(jnp.bfloat16)
    grad_w_out = outer_product(attn_low, out_grad)
    attn_grad = times_transposed(out_grad, w_out).astype(jnp.bfloat16)
    grad_query, grad_key, grad_value = attend_backward(
        query_rows, key_rows, value_rows, attn_grad, attn_raw, log_sum, local_graphs, group_graphs
    )
    qkv_grad = jnp.concatenate([grad_query, grad_key, grad_value], 1).astype(jnp.bfloat16)
    grad_w_qkv = outer_product(hidden_low, qkv_grad)
    grad_message, gain_one, shift_one = normalize_back(
        grad_mixed * silu_slope_plain(normed_one), standard_one, inv_one, norm_gains[0], node_total
    )
    shifted = denominator + GATE_EPS
    grad_numer = grad_message / shifted
    grad_denom = -grad_message * numerator / (shifted * shifted)
    numer_edge = grad_numer[edge_dst]
    grad_gate = numer_edge * source_b + grad_denom[edge_dst]
    grad_pre_edge = grad_gate * gating * (1.0 - gating)
    edge_grad = grad_pre_edge.astype(jnp.bfloat16)
    grad_w_edge = outer_product(edge_feat, edge_grad)
    grad_dest = jax.ops.segment_sum(grad_pre_edge, edge_dst, row_count)
    grad_extended = jax.ops.segment_sum(
        jnp.concatenate([numer_edge * gating, grad_pre_edge], 1),
        edge_src,
        row_count + halo_send.shape[0],
    )
    returned = return_sources(grad_extended[row_count:])
    grad_source = grad_extended[:row_count].at[halo_send].add(returned)
    proj_grad = jnp.concatenate(
        [grad_message, grad_source[:, :model_width], grad_dest, grad_source[:, model_width:]], 1
    ).astype(jnp.bfloat16)
    grad_w_proj = outer_product(hidden_low, proj_grad)
    grad_hidden = (
        grad_mixed
        + grad_two
        + times_transposed(proj_grad, w_proj)
        + times_transposed(qkv_grad, w_qkv)
    )
    weight_grads = (grad_w_proj, grad_w_edge, grad_w_qkv, grad_w_out, grad_w_up, grad_w_down)
    return (
        grad_hidden,
        weight_grads,
        jnp.stack([gain_one, gain_two, gain_three]),
        jnp.stack([shift_one, shift_two, shift_three]),
    )


def per_device(
    node_input,
    edge_feat,
    graph_ids,
    edge_src,
    edge_dst,
    halo_send,
    w_proj,
    w_edge,
    w_qkv,
    w_out,
    w_up,
    w_down,
    norm_gain,
    norm_shift,
    cotangent,
):
    group_graphs = lax.all_gather(graph_ids, "nodes", axis=0, tiled=True)
    node_total = node_input.shape[0] * lax.axis_size("nodes") * lax.axis_size("rep")
    layer_count = w_proj.shape[0]
    layer_params = [
        (
            w_proj[layer_index],
            w_edge[layer_index],
            w_qkv[layer_index],
            w_out[layer_index],
            w_up[layer_index],
            w_down[layer_index],
            norm_gain[layer_index],
            norm_shift[layer_index],
        )
        for layer_index in range(layer_count)
    ]
    hidden = node_input.astype(jnp.float32)
    saved_all = []
    for layer_index in range(layer_count):
        hidden, saved = layer_forward(
            hidden,
            layer_params[layer_index],
            edge_feat,
            edge_src,
            edge_dst,
            halo_send,
            graph_ids,
            group_graphs,
            node_total,
        )
        saved_all.append(saved)
    grad_hidden = cotangent.astype(jnp.float32)
    weight_parts = [None] * layer_count
    gain_parts = [None] * layer_count
    shift_parts = [None] * layer_count
    for layer_index in range(layer_count - 1, -1, -1):
        (
            grad_hidden,
            weight_parts[layer_index],
            gain_parts[layer_index],
            shift_parts[layer_index],
        ) = layer_backward(
            grad_hidden,
            layer_params[layer_index],
            saved_all[layer_index],
            edge_feat,
            edge_src,
            edge_dst,
            halo_send,
            graph_ids,
            group_graphs,
            node_total,
        )
    proj_local = jnp.stack([weight_parts[layer_index][0] for layer_index in range(layer_count)])
    edge_local = jnp.stack([weight_parts[layer_index][1] for layer_index in range(layer_count)])
    qkv_local = jnp.stack([weight_parts[layer_index][2] for layer_index in range(layer_count)])
    out_local = jnp.stack([weight_parts[layer_index][3] for layer_index in range(layer_count)])
    up_local = jnp.stack([weight_parts[layer_index][4] for layer_index in range(layer_count)])
    down_local = jnp.stack([weight_parts[layer_index][5] for layer_index in range(layer_count)])
    grad_proj, grad_edge, grad_qkv, grad_out, grad_up, grad_down = lax.psum(
        (proj_local, edge_local, qkv_local, out_local, up_local, down_local), ("nodes", "rep")
    )
    return (
        hidden,
        grad_hidden,
        grad_proj,
        grad_edge,
        grad_qkv,
        grad_out,
        grad_up,
        grad_down,
        jnp.stack(gain_parts),
        jnp.stack(shift_parts),
    )


def solution(mesh):
    in_specs = (
        P(("rep", "nodes"), None),
        P(("rep", "nodes"), None),
        P(("rep", "nodes")),
        P(("rep", "nodes")),
        P(("rep", "nodes")),
        P(("rep", "nodes")),
        P(),
        P(),
        P(),
        P(),
        P(),
        P(),
        P(),
        P(),
        P(("rep", "nodes"), None),
    )
    out_specs = (
        P(("rep", "nodes"), None),
        P(("rep", "nodes"), None),
        P(),
        P(),
        P(),
        P(),
        P(),
        P(),
        P(),
        P(),
    )
    N, M = mesh.shape["nodes"], mesh.shape["rep"]
    fused = N in (4, 8) and M % 2 == 0 and 512 % (16 * N * M) == 0
    return jax.shard_map(
        functools.partial(fused_device, N, M) if fused else per_device,
        mesh=mesh, in_specs=in_specs, out_specs=out_specs, check_vma=False,
    )
```

```python
import functools
import math

import jax
import jax.numpy as jnp
from jax import lax
from jax.experimental import pallas as pl
from jax.experimental.pallas import tpu as pltpu
from jax.sharding import PartitionSpec as P

HEADS = 8
HEAD_DIM = 32
NEG = -1e30
NORM_EPS = 1e-05
GATE_EPS = 1e-06
F32, BF16, I32 = jnp.float32, jnp.bfloat16, jnp.int32
MESH = pl.DeviceIdType.MESH
SYNCS = 12
STRIP = 32
GROUPS = (
    ("early", 1, 0, 2560, ("core", "y", "x", "z")),
    ("conv", 1, 0, 2560, ("core", "y", "x", "z")),
    ("qkv", 1, 0, 1536, ("core", "y", "x", "z")),
    ("early", 0, 0, 2560, ("core", "x", "y", "z")),
    ("conv", 0, 0, 2560, ("core", "y", "x", "z")),
    ("qkv", 0, 0, 1024, ("rep", "nodes")),
    ("qkv", 0, 1024, 512, ("nodes", "rep")),
)


def dot(left, right):
    return lax.dot_general(
        left, right, (((1,), (0,)), ((), ())), preferred_element_type=F32
    )


def dot_nt(left, right):
    return lax.dot_general(
        left, right, (((1,), (1,)), ((), ())), preferred_element_type=F32
    )


def dot_tn(left, right):
    return lax.dot_general(
        left, right, (((0,), (0,)), ((), ())), preferred_element_type=F32
    )


def split(value):
    high = value.astype(BF16)
    return high, (value - high.astype(F32)).astype(BF16)


def sigmoid(value):
    return jax.nn.sigmoid(value)


def silu_slope(value):
    logistic = sigmoid(value)
    return logistic * (1.0 + value * (1.0 - logistic))


def col_sum(value):
    return jnp.sum(value, axis=0, keepdims=True)


def pack(first, second):
    return jnp.concatenate([first[:, :128], first[:, 128:], second[:, :128], second[:, 128:]], 0)


def unpack(tile):
    return [jnp.concatenate([tile[i : i + 1], tile[i + 1 : i + 2]], 1) for i in (0, 2)]


def combine_moments(tiles, count):
    mean = jnp.mean(tiles[:, 0:2], 0)
    off = tiles[:, 0:2] - mean
    return jnp.concatenate([mean, jnp.sum(tiles[:, 2:4] + count * off * off, 0)], 0)


class Refs:
    pass


def axis_sizes(N, M):
    return dict(core=2, y=M // 2, x=2, z=N // 2, rep=M, nodes=N)


def scratch_list(N, M, L, R, E):
    NZ, NB, G = N // 2, N // 4, N * R
    D, FF, W, HH = 256, 512, 4 * R, HEADS // 2 * R
    dma = lambda *shape: pltpu.SemaphoreType.DMA(shape)
    vm = lambda dtype, *shape: pltpu.VMEM(shape, dtype)
    names = dict(
        gb=vm(BF16, L, N, R, D),
        xs=vm(BF16, L, N, R, D),
        meta=vm(I32, N, 8, 256),
        cot=vm(BF16, R, D),
        wp=vm(BF16, L, D, 4 * D),
        we=vm(BF16, L, D, D),
        wqkv=vm(BF16, L, D, 3 * D),
        wo=vm(BF16, L, D, D),
        wu=vm(BF16, L, D, FF),
        wd=vm(BF16, L, FF, D),
        st1=vm(F32, SYNCS, M * N, 4, 128),
        gain=vm(F32, L, 8, D),
        shift=vm(F32, L, 8, D),
        ggain=vm(F32, L, 8, D),
        gshift=vm(F32, L, 8, D),
        iv=vm(F32, L, 8, D),
        moff=vm(F32, N, 8, D),
        move=vm(F32, 8, D),
        le=vm(BF16, E, 1024),
        re=vm(BF16, 1024, D),
        TT=vm(BF16, R, 2 * E),
        ST=vm(BF16, 256, E),
        efT=vm(BF16, D, E),
        HS=vm(BF16, 64, R),
        hx=vm(BF16, L, 64, D),
        A=vm(BF16, R, 64),
        bias=vm(F32, R, G),
        xf=vm(F32, L + 1, R, D),
        xe=vm(BF16, L, 256, D),
        xeT=vm(BF16, D, 256),
        gate=vm(F32, L, E, D),
        bs=vm(BF16, L, E, D),
        num=vm(F32, L, R, D),
        den=vm(F32, L, R, D),
        z0=vm(F32, L, R, D),
        z1=vm(F32, L, R, D),
        z2=vm(F32, L, R, D),
        wkvT=vm(BF16, L, 2 * D, D),
        kvT=vm(BF16, L, 2 * D, G),
        odT=vm(F32, NB, D, R),
        ldT=vm(F32, NB, D, R),
        md=vm(F32, NB, R, D),
        rb=vm(F32, L, NB, R, D),
        pst=vm(BF16, L, HEADS * R, G),
        oraw=vm(F32, L, R, D),
        ob=vm(BF16, L, R, D),
        mb=vm(BF16, L, R, D),
        u=vm(F32, L, R, FF),
        g=vm(BF16, L, R, FF),
        dy=vm(F32, R, D),
        dmix=vm(F32, R, D),
        gy0=vm(F32, R, D),
        local=vm(F32, R, D),
        dxo=vm(F32, R, D),
        dob=vm(F32, R, D),
        dqT=vm(F32, D, R),
        qm=vm(BF16, L, 2, HH, 128),
        q=vm(BF16, L, R, D),
        qT=vm(BF16, D, R),
        dosT=vm(BF16, 128, R),
        dom=vm(BF16, HH, 256),
        sc=vm(F32, 2, max(2 * R, E), W),
        tp=vm(F32, HEADS // 2, R, 128),
        dss=vm(BF16, HH, W),
        dkv=vm(BF16, 2 * D, W),
        gkv=vm(F32, 2 * D, D),
        gg=vm(BF16, 2 * E, 2 * D),
        dn=vm(BF16, 512, 2 * D),
        dproj=vm(BF16, 256, 4 * D),
        dxs=vm(BF16, L, NZ, 2, R, D),
        rs1=vm(BF16, L, NZ, R, D),
        cs=vm(BF16, L, NZ, R, D),
        rs2=vm(BF16, L, NZ, R, D),
        ro=vm(BF16, L, 3, R, D),
        hs=vm(BF16, L, 2, 32, D),
        hr=vm(BF16, L, 2, 32, D),
    )
    names.update(
        gs_early=vm(BF16, L, 2560, 128),
        gs_conv=vm(BF16, L, 2560, 128),
        gs_qkv=vm(BF16, L, 1536, 128),
    )
    sizes = axis_sizes(N, M)
    for g, (_, _, _, rows, stages) in enumerate(GROUPS):
        names[f"go{g}"] = vm(BF16, rows, 128)
        left = rows
        for k, axis in enumerate(stages):
            left //= sizes[axis]
            names[f"ga{g}_{k}"] = vm(BF16, sizes[axis] - 1, left, 128)
            if k < len(stages) - 1:
                names[f"gh{g}_{k}"] = vm(BF16, left, 128)
    names.update(
        ar_s=dma(len(GROUPS)),
        ar_r=dma(sum(2 * len(stages) for *_, stages in GROUPS)),
        ar_l=dma(len(GROUPS)),
        load=dma(9),
        store=dma(2),
        meta_s=dma(1),
        meta_r=dma(1),
        st_s=dma(1),
        st_r=dma(SYNCS),
        ag_s=dma(1),
        agn_r=dma(L),
        agc_r=dma(L, NZ),
        agp_r=dma(L),
        rs_s=dma(1),
        rsp_r=dma(L, NB, 2),
        ro_r=dma(L),
        rsc_r=dma(L),
        hx_s=dma(1),
        hx_r=dma(L),
        hal_s=dma(1),
        hal_r=dma(L),
    )
    return names


IN_NAMES = (
    "x_in", "ids", "edge_src", "edge_dst", "halo", "ef_h", "wp_h", "we_h", "wqkv_h", "wo_h", "wu_h", "wd_h",
    "gain_in", "shift_in", "cot_h",
)
OUT_NAMES = ("out_act", "grad_in", *(f"gout{g}" for g in range(len(GROUPS))), "ggain_out", "gshift_out")


def kernel(N, M, L, names, *args):
    r_ = Refs()
    for name, ref in zip(IN_NAMES + OUT_NAMES + tuple(names), args, strict=True):
        setattr(r_, name, ref)
    R, D = r_.x_in.shape
    E = r_.ef_h.shape[0]
    NZ, NB, G, W = N // 2, N // 4, N * R, 4 * R
    HK = HEADS // 2
    total = float(N * M * R)
    scale = HEAD_DIM ** -0.5
    me = lax.axis_index("nodes")
    rep = lax.axis_index("rep")
    z = me // 2
    par = me % 2
    partner = 2 * z + (1 - par)
    prev = (me + N - 1) % N
    nxt = (me + 1) % N
    zh, zl = z // 2, z % 2
    z_to = lambda t: 2 * ((zh + t // 2) % NB) + (zl + t % 2) % 2
    z_from = lambda t: 2 * ((zh + NB - t // 2) % NB) + (zl + t % 2) % 2

    def remote(src, dst, s_sem, r_sem, **where):
        return pltpu.make_async_remote_copy(
            src_ref=src, dst_ref=dst, send_sem=s_sem, recv_sem=r_sem,
            device_id=where, device_id_type=MESH,
        )

    def send(src, dst, s_sem, r_sem, **where):
        remote(src, dst, s_sem, r_sem, **where).start()

    def send_rows(src, dst, rows, s_sem, r_sem, **where):
        pieces = next(p for p in range(1, rows) if rows % (16 * p) == 0 and rows // p <= 128)
        for at in range(0, rows, rows // pieces):
            cut = pl.ds(at, rows // pieces)
            send(src.at[cut], dst.at[cut], s_sem, r_sem, **where)

    def arrive(dst, r_sem):
        remote(dst, dst, r_sem, r_sem, nodes=partner).wait_recv()

    def sent(src, s_sem):
        remote(src, src, s_sem, s_sem, nodes=partner).wait_send()

    def when(condition, *acts):
        if condition:
            for act in acts:
                act()

    loads = [pltpu.make_async_copy(r_.ef_h, r_.le.at[:, D : 2 * D], r_.load.at[0])] + [
        pltpu.make_async_copy(getattr(r_, f"{name}_h"), getattr(r_, name), r_.load.at[1 + i])
        for i, name in enumerate(("we", "wqkv", "wp", "wo", "wu", "wd", "cot"))
    ]
    own_rows = pltpu.make_async_copy(r_.x_in, r_.gb.at[0, me], r_.load.at[8])
    own_rows.start()
    for load in loads:
        load.start()

    barrier = pltpu.get_barrier_semaphore()
    for dr in range(M):
        for d in range(N):
            if dr + d > 0:
                pl.semaphore_signal(barrier, inc=1, device_id={"rep": (rep + dr) % M, "nodes": (me + d) % N},
                                    device_id_type=MESH)
    pl.semaphore_wait(barrier, M * N - 1)

    def gather_start(l):
        mine = r_.gb.at[l, me]
        for t in range(2, NZ):
            send_rows(mine, mine, R, r_.ag_s.at[0], r_.agc_r.at[l, t], nodes=2 * z_to(t) + par)
        send_rows(mine, mine, R, r_.ag_s.at[0], r_.agn_r.at[l], nodes=partner)
        send_rows(mine, mine, R, r_.ag_s.at[0], r_.agn_r.at[l], nodes=2 * z_to(1) + par)
        send_rows(mine, mine, R, r_.ag_s.at[0], r_.agn_r.at[l], nodes=2 * z_to(1) + 1 - par)

    def gather_pass(l, t):
        piece = r_.gb.at[l, 2 * z_from(t) + par]
        arrive(piece, r_.agc_r.at[l, t])
        send_rows(piece, piece, R, r_.ag_s.at[0], r_.agp_r.at[l], nodes=partner)

    def gather_near(l):
        arrive(r_.gb.at[l, 0:3], r_.agn_r.at[l])

    def gather_far(l):
        arrive(r_.gb.at[l, 0 : NZ - 2], r_.agp_r.at[l])

    def sync_start(k, first, second):
        mine = rep * N + me
        r_.st1[k, mine] = pack(first, second)
        for dr in range(M):
            for d in range(N):
                if dr + d > 0:
                    send(r_.st1.at[k, mine], r_.st1.at[k, mine], r_.st_s.at[0], r_.st_r.at[k],
                         rep=(rep + dr) % M, nodes=(me + d) % N)

    def sync_wait(k):
        arrive(r_.st1.at[k, 0 : M * N - 1], r_.st_r.at[k])

    def sync_moments(k):
        sync_wait(k)
        return unpack(combine_moments(r_.st1[k], float(R)))

    def sync_sums(k):
        sync_wait(k)
        return unpack(jnp.sum(r_.st1[k], 0))

    sizes = axis_sizes(N, M)
    core, row = rep % 2, rep // 2
    places = dict(
        core=(core, lambda t: dict(rep=2 * row + t)),
        y=(row, lambda t: dict(rep=2 * t + core)),
        x=(par, lambda t: dict(nodes=2 * z + t)),
        z=(z, lambda t: dict(nodes=2 * t + par)),
        rep=(rep, lambda t: dict(rep=t)),
        nodes=(me, lambda t: dict(nodes=t)),
    )

    def reduce_step(g, step):
        name, layer, first, rows, stages = GROUPS[g]
        K = len(stages)
        base = sum(2 * len(before) for *_, before in GROUPS[:g])
        gs, out = getattr(r_, f"gs_{name}").at[layer, first : first + rows], getattr(r_, f"go{g}")
        count, offset = [rows], [0]
        for axis in stages:
            count.append(count[-1] // sizes[axis])
            offset.append(offset[-1] + places[axis][0] * count[-1])
        take = lambda start, size: pl.ds(pl.multiple_of(start, 16), size)
        if 1 <= step <= K:
            k = step - 1
            got = getattr(r_, f"ga{g}_{k}")
            arrive(got, r_.ar_r.at[base + k])
            held = gs if k == 0 else getattr(r_, f"gh{g}_{k - 1}")
            index = places[stages[k]][0]
            acc = held[take(index * count[k + 1], count[k + 1])].astype(F32)
            for slot in range(sizes[stages[k]] - 1):
                acc = acc + got[slot].astype(F32)
            if step < K:
                getattr(r_, f"gh{g}_{k}")[...] = acc.astype(BF16)
            else:
                out[take(offset[K], count[K])] = acc.astype(BF16)
        elif step > K:
            k = 2 * K - step
            arrive(out.at[0 : (sizes[stages[k]] - 1) * count[k + 1]], r_.ar_r.at[base + step - 1])
        if step < K:
            held = gs if step == 0 else getattr(r_, f"gh{g}_{step - 1}")
            index, device = places[stages[step]]
            size = sizes[stages[step]]
            for d in range(1, size):
                to = (index + d) % size
                send_rows(held.at[take(to * count[step + 1], count[step + 1])], getattr(r_, f"ga{g}_{step}").at[d - 1],
                     count[step + 1], r_.ar_s.at[g], r_.ar_r.at[base + step], **device(to))
        elif step < 2 * K:
            k = 2 * K - 1 - step
            index, device = places[stages[k]]
            size = sizes[stages[k]]
            here = out.at[take(offset[k + 1], count[k + 1])]
            for d in range(1, size):
                send_rows(here, here, count[k + 1], r_.ar_s.at[g], r_.ar_r.at[base + step],
                          **device((index + d) % size))
        else:
            pltpu.make_async_copy(out, getattr(r_, f"gout{g}"), r_.ar_l.at[g]).start()

    def reduce_drain(g):
        name, _, _, rows, _ = GROUPS[g]
        sent(getattr(r_, f"gs_{name}").at[:, 0 : rows - rows // (M * N)], r_.ar_s.at[g])
        pltpu.make_async_copy(getattr(r_, f"go{g}"), getattr(r_, f"gout{g}"), r_.ar_l.at[g]).wait()

    def put(buf, l, at, value):
        rows = value.shape[0]
        for c in range(value.shape[1] // 128):
            buf[l, at : at + rows] = value[:, 128 * c : 128 * (c + 1)].astype(BF16)
            at += rows
        return at

    lane_head = lax.broadcasted_iota(I32, (R, 128), 1) // HEAD_DIM

    def by_head(parts):
        out = parts[0]
        for k in range(1, HK):
            out = jnp.where(lane_head == k, parts[k], out)
        return out

    r_.meta[me] = jnp.full((8, 256), -1, I32)
    r_.meta[me, 0:1, 0:R] = r_.ids[...].reshape(1, R)
    r_.meta[me, 1:2, 0:48] = r_.halo[...].reshape(1, 48)
    for d in range(1, N):
        send(r_.meta.at[me], r_.meta.at[me], r_.meta_s.at[0], r_.meta_r.at[0], nodes=(me + d) % N)
    own_rows.wait()
    gather_start(0)

    src_row = r_.edge_src[...].reshape(1, E)
    src_row = jnp.where(src_row < R + 24, src_row, src_row + 8)
    dst_row = r_.edge_dst[...].reshape(1, E)
    src_col = jnp.broadcast_to(src_row, (128, E)).T[:, 0:1]
    dst_col = jnp.broadcast_to(dst_row, (128, E)).T[:, 0:1]
    as_mask = lambda cond: cond.astype(F32).astype(BF16)
    r_.le[:, 0:256] = as_mask(src_col == lax.broadcasted_iota(I32, (E, 256), 1))
    target = as_mask(dst_col == lax.broadcasted_iota(I32, (E, 256), 1))
    r_.le[:, 512:768] = target
    r_.le[:, 768:1024] = target
    target = as_mask(dst_row == lax.broadcasted_iota(I32, (R, E), 0))
    r_.TT[:, 0:E] = target
    r_.TT[:, E:] = target
    r_.ST[...] = as_mask(src_row == lax.broadcasted_iota(I32, (256, E), 0))
    r_.dn[R:256] = jnp.zeros((256 - R, 2 * D), BF16)
    r_.dn[256 + R : 512] = jnp.zeros((256 - R, 2 * D), BF16)
    r_.dproj[R:256, 0:D] = jnp.zeros((256 - R, D), BF16)
    r_.dproj[R:256, 2 * D : 3 * D] = jnp.zeros((256 - R, D), BF16)
    halo_col = jnp.broadcast_to(r_.meta[me][1:2, 0:128], (128, 128)).T
    hot = (halo_col[0:48, 0:1] == lax.broadcasted_iota(I32, (48, R), 1)).astype(F32)
    pad = jnp.zeros((8, R), F32)
    r_.HS[...] = jnp.concatenate([hot[0:24], pad, hot[24:48], pad], 0).astype(BF16)
    loads[0].wait()
    r_.efT[...] = r_.le[:, D : 2 * D].T
    for l in range(L):
        for k in range(3):
            r_.gain[l, k : k + 1] = r_.gain_in[k, l : l + 1]
            r_.shift[l, k : k + 1] = r_.shift_in[k, l : l + 1]
    r_.xf[0] = r_.gb[0, me].astype(F32)
    r_.moff[...] = jnp.zeros((N, 8, D), F32)
    r_.move[0:1] = jnp.ones((1, D), F32)
    r_.move[1:2] = jnp.zeros((1, D), F32)
    for load in loads[1:]:
        load.wait()
    for l in range(L):
        r_.wkvT[l] = r_.wqkv[l, :, D:].T

    arrive(r_.meta.at[0 : N - 1], r_.meta_r.at[0])
    id_col = jnp.broadcast_to(r_.meta[me][0:1, 0:R], (128, R)).T[:, 0:1]
    id_row = jnp.concatenate(
        [r_.meta[4 * ((zh + NB - j // 4) % NB) + j % 4][0:1, 0:R] for j in range(N)], 1
    )
    r_.bias[...] = jnp.where(id_col == id_row, 0.0, NEG)

    r_.A[...] = as_mask(r_.meta[me][1:2, 0:64] == lax.broadcasted_iota(I32, (R, 64), 0))

    factor_exp = scale * math.log2(math.e)

    def prepare_queries(l):
        q = dot(r_.xs[l, me], r_.wqkv[l, :, :D]).astype(BF16)
        r_.q[l] = q
        q = q.astype(F32)
        for hf in range(2):
            for k in range(HK):
                part = jnp.where(lane_head == k, q[:, 128 * hf : 128 * (hf + 1)], 0.0)
                r_.qm[l, hf, k * R : (k + 1) * R] = part.astype(BF16)

    def head_dims(hf, k, base=0):
        first = base + hf * 128 + k * HEAD_DIM
        return slice(first, first + HEAD_DIM)

    def head_rows(hf, k, count=1):
        return slice((hf * HK + k) * R, (hf * HK + k + count) * R)

    def lane_half(hf):
        return slice(hf * 128, (hf + 1) * 128)

    def half_of(i):
        return (zh + NB - i) % NB, slice(i * W, (i + 1) * W)

    def attention_keys(l, i):
        half, rows = half_of(i)
        x = r_.xs[l, pl.ds(4 * half, 4)].reshape(W, D)
        r_.kvT[l, :, rows] = dot_nt(r_.wkvT[l], x).astype(BF16)

    def attention_heads(l, i, hfs):
        _, rows = half_of(i)
        for hf in hfs:
            lanes = lane_half(hf)
            ones = jnp.ones((HEAD_DIM, W), BF16)
            for c in range(HK // 2):
                r_.sc[c % 2, 0 : 2 * R] = dot(r_.qm[l, hf, 2 * c * R : 2 * (c + 1) * R], r_.kvT[l, lanes, rows])
                for k in range(2):
                    for at in range(0, R, STRIP):
                        s = r_.sc[c % 2, k * R + at : k * R + at + STRIP] + r_.bias[at : at + STRIP, rows]
                        top = jnp.max(s, 1, keepdims=True)
                        e = jnp.exp2((s - top) * factor_exp)
                        r_.tp[2 * c + k, at : at + STRIP] = jnp.broadcast_to(top, (STRIP, 128))
                        first = (hf * HK + 2 * c + k) * R + at
                        r_.pst[l, first : first + STRIP, rows] = e.astype(BF16)
                for k in range(2):
                    h = 2 * c + k
                    left = jnp.concatenate([r_.kvT[l, head_dims(hf, h, D), rows], ones], 0)
                    o = dot_nt(left, r_.pst[l, head_rows(hf, h), rows])
                    r_.odT[i, head_dims(hf, h)] = o[0:HEAD_DIM]
                    r_.ldT[i, head_dims(hf, h)] = o[HEAD_DIM:]
            r_.md[i, :, lanes] = by_head([r_.tp[k] for k in range(HK)])

    def attention_end(l):
        tops = [r_.md[i].T for i in range(NB)]
        top = tops[0]
        for i in range(1, NB):
            top = jnp.maximum(top, tops[i])
        factors = [jnp.exp2((tops[i] - top) * factor_exp) for i in range(NB)]
        inv = 1.0 / sum(factors[i] * r_.ldT[i] for i in range(NB))
        o = jnp.zeros((D, R), F32)
        for i in range(NB):
            r_.rb[l, i] = (factors[i] * inv).T
            o = o + factors[i] * inv * r_.odT[i]
        o = o.T
        r_.oraw[l] = o
        ob = o.astype(BF16)
        r_.ob[l] = ob
        t1 = r_.xf[l] + dot(ob, r_.wo[l])
        r_.z1[l] = t1
        mean1 = col_sum(t1) / R
        return mean1, col_sum((t1 - mean1) * (t1 - mean1))

    def convolution(l):
        xs = r_.xs
        xb = xs[l, me]
        r_.xe[l, 0:R] = xb
        arrive(r_.xe.at[l, R : R + 64], r_.hx_r.at[l])
        xe = r_.xe[l]
        made = dot(xe, r_.wp[l])
        pd_high, pd_low = split(made[:, 2 * D : 3 * D])
        r_.re[0:256] = made[:, 3 * D :].astype(BF16)
        r_.re[256:512] = r_.we[l]
        r_.re[512:768] = pd_high
        r_.re[768:1024] = pd_low
        r_.gate[l] = dot(r_.le[...], r_.re[...])
        r_.bs[l] = dot(r_.le[:, 0:256], made[:, D : 2 * D].astype(BF16)).astype(BF16)
        for at in range(0, E, 64):
            here = slice(at, at + 64)
            gate = sigmoid(r_.gate[l, here])
            r_.gate[l, here] = gate
            high, low = split(jnp.concatenate([gate * r_.bs[l, here].astype(F32), gate], 1))
            r_.gg[here] = high
            r_.gg[E + at : E + at + 64] = low
        num_den = dot(r_.TT[...], r_.gg[...])
        pa, num, den = made[0:R, 0:D], num_den[:, 0:D], num_den[:, D:]
        r_.num[l] = num
        r_.den[l] = den
        msg = pa + num / (den + GATE_EPS)
        r_.z0[l] = msg
        mean0 = col_sum(msg) / R
        return mean0, col_sum((msg - mean0) * (msg - mean0))

    def forward(l):
        def ready(js):
            for j in js:
                moved = (r_.gb[l, j].astype(F32) + r_.moff[j, 0:1]) * r_.move[0:1] + r_.move[1:2]
                r_.xs[l, j] = moved.astype(BF16)

        r_.xs[l, me] = r_.xf[l].astype(BF16)
        r_.hx[l] = dot(r_.HS[...], r_.xs[l, me]).astype(BF16)
        send(r_.hx.at[l, 0:32], r_.xe.at[l, R + 32 : R + 64], r_.hx_s.at[0], r_.hx_r.at[l], nodes=prev)
        send(r_.hx.at[l, 32:64], r_.xe.at[l, R : R + 32], r_.hx_s.at[0], r_.hx_r.at[l], nodes=nxt)
        prepare_queries(l)
        for t in range(2, NZ):
            gather_pass(l, t)
        mean0, sq0 = convolution(l)
        sync_start(3 * l, mean0, sq0)
        gather_near(l)
        ready([partner, 2 * z_from(1) + par, 2 * z_from(1) + 1 - par])

        attention_keys(l, 0)
        attention_heads(l, 0, (0, 1))
        gather_far(l)
        ready([2 * z_from(t) + p for t in range(2, NZ) for p in range(2)])
        for i in range(1, NB):
            attention_keys(l, i)
            attention_heads(l, i, (0, 1))
        mean1, sq1 = attention_end(l)
        sync_start(3 * l + 1, mean1, sq1)
        mean0, sq0 = sync_moments(3 * l)
        inv0 = lax.rsqrt(sq0 / total + NORM_EPS)
        r_.iv[l, 0:1] = inv0
        z0 = (r_.z0[l] - mean0) * inv0
        r_.z0[l] = z0
        n0 = z0 * r_.gain[l, 0:1] + r_.shift[l, 0:1]
        r_.local[...] = r_.xf[l] + n0 * sigmoid(n0)
        mean1, sq1 = sync_moments(3 * l + 1)
        inv1 = lax.rsqrt(sq1 / total + NORM_EPS)
        r_.iv[l, 1:2] = inv1
        z1 = (r_.z1[l] - mean1) * inv1
        r_.z1[l] = z1
        mix = r_.local[...] + z1 * r_.gain[l, 1:2] + r_.shift[l, 1:2]
        mb = mix.astype(BF16)
        r_.mb[l] = mb
        u = dot(mb, r_.wu[l])
        r_.u[l] = u
        g = (u * sigmoid(u)).astype(BF16)
        r_.g[l] = g
        y = mix + dot(g, r_.wd[l])
        r_.z2[l] = y
        mean = col_sum(y) / R
        cent = y - mean
        k = 3 * l + 2
        sync_start(k, mean, col_sum(cent * cent))

        if l < L - 1:
            r_.gb[l + 1, me] = cent.astype(BF16)
            gather_start(l + 1)

        if l == L - 1:
            dy = r_.cot[...].astype(F32)
            sync_start(3 * L, col_sum(dy), col_sum(dy * cent))

        tot_mean, tot_sq = sync_moments(k)
        inv2 = lax.rsqrt(tot_sq / total + NORM_EPS)
        r_.iv[l, 2:3] = inv2
        z2 = (r_.z2[l] - tot_mean) * inv2
        r_.z2[l] = z2
        gain, shift = r_.gain[l, 2:3], r_.shift[l, 2:3]
        r_.xf[l + 1] = z2 * gain + shift

        if l == L - 1:
            sync_wait(3 * L)
            sums, means = r_.st1[3 * L], r_.st1[k][:, 0:2]
            mean = jnp.mean(means, 0)
            dy_sum = jnp.sum(sums[:, 0:2], 0)
            dy_cent = jnp.sum(sums[:, 2:4] + (means - mean) * sums[:, 0:2], 0)
            dy_sum, dy_cent = unpack(jnp.concatenate([dy_sum, dy_cent], 0))
            r_.gshift[l, 2:3] = dy_sum
            r_.ggain[l, 2:3] = dy_cent * inv2

        for j in range(N):
            tile = r_.st1[k, rep * N + j]
            r_.moff[j, 0:1] = jnp.concatenate([tile[0:1], tile[1:2]], 1) - tot_mean
        r_.move[0:1] = inv2 * gain
        r_.move[1:2] = shift

    for l in range(L):
        forward(l)
    act_copy = pltpu.make_async_copy(r_.xf.at[L], r_.out_act, r_.store.at[0])
    act_copy.start()

    def back_feed_forward(l, k):
        s2, g2 = r_.gshift[l, 2:3], r_.ggain[l, 2:3]
        d3 = r_.gain[l, 2:3] * r_.iv[l, 2:3] * (r_.dy[...] - s2 / total - r_.z2[l] * (g2 / total))
        db = d3.astype(BF16)
        dub = (dot_nt(db, r_.wd[l]) * silu_slope(r_.u[l])).astype(BF16)
        dmix = d3 + dot_nt(dub, r_.wu[l])
        r_.dmix[...] = dmix
        n0 = r_.z0[l] * r_.gain[l, 0:1] + r_.shift[l, 0:1]
        gy0 = dmix * silu_slope(n0)
        sync_start(k, col_sum(dmix), col_sum(dmix * r_.z1[l]))
        sync_start(k + 1, col_sum(gy0), col_sum(gy0 * r_.z0[l]))
        r_.gy0[...] = gy0
        at = put(r_.gs_early, l, 512, dot_tn(r_.mb[l], dub))
        put(r_.gs_early, l, at, dot_tn(r_.g[l], db))
        r_.xeT[...] = r_.xe[l].T
        r_.qT[...] = r_.q[l].T

    def back_norms(l, k):
        s1, g1 = sync_sums(k)
        r_.gshift[l, 1:2] = s1
        r_.ggain[l, 1:2] = g1
        dmix = r_.dmix[...]
        d2 = r_.gain[l, 1:2] * r_.iv[l, 1:2] * (dmix - s1 / total - r_.z1[l] * (g1 / total))
        dab = d2.astype(BF16)
        r_.dxo[...] = dmix + d2
        r_.dob[...] = dot_nt(dab, r_.wo[l]).astype(BF16).astype(F32)
        put(r_.gs_early, l, 0, dot_tn(r_.ob[l], dab))
        r_.gkv[...] = jnp.zeros((2 * D, D), F32)
        r_.dqT[...] = jnp.zeros((D, R), F32)

    def back_half(i):
        t1 = (i + 1) % NB
        half = (zh + t1) % NB
        place = (NB - t1) % NB
        return place, half, slice(place * W, (place + 1) * W)

    def back_heads(l, i, hf):
        place, half, rows = back_half(i)
        if True:
            lanes = lane_half(hf)
            dos = r_.dob[:, lanes] * r_.rb[l, place, :, lanes]
            prod = dos * r_.oraw[l, :, lanes]
            for k in range(HK):
                r_.dom[k * R : (k + 1) * R, 0:128] = jnp.where(lane_head == k, dos, 0.0).astype(BF16)
                r_.dom[k * R : (k + 1) * R, 128:256] = jnp.where(lane_head == k, -prod, 0.0).astype(BF16)
            r_.dosT[...] = dos.T.astype(BF16)
            values = slice(D + hf * 128, D + (hf + 1) * 128)
            right = jnp.concatenate([r_.kvT[l, values, rows], jnp.ones((128, W), BF16)], 0)
            for c in range(HK // 2):
                both = slice(2 * c * R, 2 * (c + 1) * R)
                r_.sc[c % 2, 0 : 2 * R] = dot(r_.dom[both], right)
                for k in range(2):
                    for at in range(0, R, STRIP):
                        first = (hf * HK + 2 * c + k) * R + at
                        e = r_.pst[l, first : first + STRIP, rows].astype(F32)
                        ds = e * r_.sc[c % 2, k * R + at : k * R + at + STRIP]
                        r_.dss[(2 * c + k) * R + at : (2 * c + k) * R + at + STRIP] = ds.astype(BF16)
                for k in range(2):
                    h = 2 * c + k
                    mine, dims = slice(h * R, (h + 1) * R), head_dims(hf, h)
                    r_.dqT[dims] += dot_nt(r_.kvT[l, dims, rows], r_.dss[mine])
                    r_.dkv[dims] = (dot(r_.qT[dims], r_.dss[mine]) * scale).astype(BF16)
                    dv = dot(r_.dosT[h * HEAD_DIM : (h + 1) * HEAD_DIM], r_.pst[l, head_rows(hf, h), rows])
                    r_.dkv[head_dims(hf, h, D)] = dv.astype(BF16)

    def back_rows(l, i):
        _, half, _ = back_half(i)
        dx = dot(r_.wqkv[l, :, D:], r_.dkv[...]).T
        r_.dxs[l, pl.ds(2 * half, 2)] = dx.astype(BF16).reshape(2, 2, R, D)

        if i < NB - 1:
            for t in (2 * (i + 1), 2 * (i + 1) + 1):
                zb = z_to(t)
                send_rows(r_.dxs.at[l, zb, 1 - par], r_.rs1.at[l, zb], R,
                          r_.rs_s.at[0], r_.rsp_r.at[l, i, t % 2], nodes=partner)

        else:
            near = z_to(1)
            send_rows(r_.dxs.at[l, z, 1 - par], r_.ro.at[l, 0], R, r_.rs_s.at[0], r_.ro_r.at[l], nodes=partner)
            send_rows(r_.dxs.at[l, near, par], r_.ro.at[l, 1], R, r_.rs_s.at[0], r_.ro_r.at[l], nodes=2 * near + par)
            send_rows(r_.dxs.at[l, near, 1 - par], r_.ro.at[l, 2], R, r_.rs_s.at[0], r_.ro_r.at[l],
                 nodes=2 * near + 1 - par)

        r_.gkv[...] += dot(r_.dkv[...], r_.xs[l, pl.ds(4 * half, 4)].reshape(W, D))

    def pass_on(l, i, t):
        zb = z_to(t)
        arrive(r_.rs1.at[l, zb], r_.rsp_r.at[l, i, t % 2])
        both = r_.dxs[l, zb, par].astype(F32) + r_.rs1[l, zb].astype(F32)
        r_.cs[l, zb] = both.astype(BF16)
        send_rows(r_.cs.at[l, zb], r_.rs2.at[l, z], R, r_.rs_s.at[0], r_.rsc_r.at[l], nodes=2 * zb + par)

    def back_convolution(l, k):
        s0, g0 = unpack(jnp.sum(r_.st1[k + 1], 0))
        r_.gshift[l, 0:1] = s0
        r_.ggain[l, 0:1] = g0
        inv_den = 1.0 / (r_.den[l] + GATE_EPS)
        dm = r_.gain[l, 0:1] * r_.iv[l, 0:1] * (r_.gy0[...] - s0 / total - r_.z0[l] * (g0 / total))
        dnum = dm * inv_den
        dden = -dnum * r_.num[l] * inv_den
        high, low = split(jnp.concatenate([dnum, dden], 1))
        r_.dn[0:R] = high
        r_.dn[256 : 256 + R] = low
        r_.sc[0, 0:E, 0 : 2 * D] = dot(r_.le[:, 512:1024], r_.dn[...])
        for at in range(0, E, 64):
            here = slice(at, at + 64)
            gate, dnum_e = r_.gate[l, here], r_.sc[0, here, 0:D]
            dgp = (dnum_e * r_.bs[l, here].astype(F32) + r_.sc[0, here, D : 2 * D]) * gate * (1.0 - gate)
            r_.gg[here, 0:D] = (dnum_e * gate).astype(BF16)
            r_.gg[here, D:] = dgp.astype(BF16)
        ext = dot(r_.ST[...], r_.gg[0:E]).astype(BF16)
        r_.dproj[0:R, 0:D] = dm.astype(BF16)
        r_.dproj[:, D : 2 * D] = ext[:, 0:D]
        r_.dproj[0:R, 2 * D : 3 * D] = dot(r_.TT[:, 0:E], r_.gg[0:E, D:]).astype(BF16)
        r_.dproj[:, 3 * D :] = ext[:, D:]
        dxe = dot_nt(r_.dproj[...], r_.wp[l])
        r_.hs[l, 0] = dxe[R : R + 32].astype(BF16)
        r_.hs[l, 1] = dxe[R + 32 : R + 64].astype(BF16)
        r_.dxo[...] += dxe[0:R]

    def send_halo(l):
        send(r_.hs.at[l, 0], r_.hr.at[l, 1], r_.hal_s.at[0], r_.hal_r.at[l], nodes=prev)
        send(r_.hs.at[l, 1], r_.hr.at[l, 0], r_.hal_s.at[0], r_.hal_r.at[l], nodes=nxt)

    def conv_weight_grads(l):
        at = put(r_.gs_conv, l, 0, dot(r_.xeT[...], r_.dproj[...]))
        put(r_.gs_conv, l, at, dot(r_.efT[...], r_.gg[0:E, D:]))

    def back_input(l):
        dx = r_.dxo[...]
        dx = dx + r_.dxs[l, z, par].astype(F32)
        arrive(r_.ro.at[l], r_.ro_r.at[l])
        for slot in range(3):
            dx = dx + r_.ro[l, slot].astype(F32)
        if NZ > 2:
            arrive(r_.rs2.at[l, 0 : NZ - 2], r_.rsc_r.at[l])
        for t in range(2, NZ):
            dx = dx + r_.rs2[l, z_from(t)].astype(F32)
        arrive(r_.hr.at[l], r_.hal_r.at[l])
        back = jnp.concatenate(
            [r_.hr[l, 0].astype(F32)[0:24], r_.hr[l, 1].astype(F32)[0:24], jnp.zeros((16, D), F32)], 0
        )
        return dx + dot(r_.A[...], back.astype(BF16))

    r_.dy[...] = r_.cot[...].astype(F32)

    E1, C1, Q1, E0, C0, QK0, V0 = range(len(GROUPS))

    def steps(*pairs):
        return [functools.partial(reduce_step, g, k) for g, k in pairs]

    r_.dy[...] = r_.cot[...].astype(F32)

    def backward(b):
        l = L - 1 - b
        first, last = b == 0, b == L - 1
        k = 3 * L + 1 + 2 * b
        back_feed_forward(l, k)
        when(last, *steps((E1, 4), (C1, 4), (Q1, 2)))
        back_norms(l, k)
        if first:
            when(True, *steps((E1, 0)))
            back_heads(l, 0, 0)
            back_heads(l, 0, 1)
            back_rows(l, 0)
            when(True, *steps((E1, 1)))
            sync_wait(k + 1)
            back_convolution(l, k)
            send_halo(l)
            pass_on(l, 0, 2)
            conv_weight_grads(l)
            when(True, *steps((C1, 0)))
            back_heads(l, 1, 0)
            pass_on(l, 0, 3)
            when(True, *steps((C1, 1)))
            back_heads(l, 1, 1)
            back_rows(l, 1)
        else:
            when(True, *steps((E1, 5), (C1, 5), (Q1, 3), (E0, 0)))
            sync_wait(k + 1)
            back_convolution(l, k)
            send_halo(l)
            when(True, *steps((E0, 1)))
            conv_weight_grads(l)
            when(True, *steps((C0, 0), (E1, 6), (C1, 6), (Q1, 4)))
            back_heads(l, 0, 0)
            when(True, *steps((C0, 1)))
            back_heads(l, 0, 1)
            back_rows(l, 0)
            when(True, *steps((E0, 2), (E1, 7), (C1, 7), (Q1, 5)))
            back_heads(l, 1, 0)
            when(True, *steps((E0, 3), (C0, 2), (E1, 8), (C1, 8), (Q1, 6)))
            for t in range(2, NZ):
                pass_on(l, 0, t)
            back_heads(l, 1, 1)
            back_rows(l, 1)
            when(True, *steps((E0, 4), (C0, 3), (Q1, 7)))
        dqb = (r_.dqT[...].T * scale).astype(BF16)
        r_.dxo[...] += dot_nt(dqb, r_.wqkv[l, :, 0:D])
        at = put(r_.gs_qkv, l, 0, dot(r_.xeT[:, 0:R], dqb))
        put(r_.gs_qkv, l, at, r_.gkv[...].T)
        if first:
            when(True, *steps((Q1, 0)))
            dx = back_input(l)
            r_.dy[...] = dx
            below = L - 2
            sync_start(SYNCS - 1, col_sum(dx), col_sum(dx * r_.z2[below]))
            when(True, *steps((E1, 2), (C1, 2), (Q1, 1)))
            s2, g2 = sync_sums(SYNCS - 1)
            r_.gshift[below, 2:3] = s2
            r_.ggain[below, 2:3] = g2
            when(True, *steps((E1, 3), (C1, 3)))

    for b in range(L):
        backward(b)
    for step in steps((QK0, 0), (V0, 0), (E0, 5), (C0, 4), (V0, 1), (QK0, 1), (Q1, 8)):
        step()
    r_.dy[...] = back_input(0)
    in_copy = pltpu.make_async_copy(r_.dy, r_.grad_in, r_.store.at[1])
    in_copy.start()
    for step in steps(
        (E0, 6), (C0, 5), (V0, 2), (QK0, 2),
        (E0, 7), (C0, 6), (V0, 3), (QK0, 3),
        (E0, 8), (C0, 7), (V0, 4), (QK0, 4), (C0, 8),
    ):
        step()
    for l in range(L):
        for k in range(3):
            r_.ggain_out[k, l : l + 1] = r_.ggain[l, k : k + 1]
            r_.gshift_out[k, l : l + 1] = r_.gshift[l, k : k + 1]
    for g in range(len(GROUPS)):
        reduce_drain(g)
    sent(r_.meta.at[0 : N - 1], r_.meta_s.at[0])
    sent(r_.st1.at[:, 0 : M * N - 1], r_.st_s.at[0])
    sent(r_.gb.at[:, 0 : 3 + 2 * (NZ - 2)], r_.ag_s.at[0])
    sent(r_.gb.at[:, 0 : 2 * (NB - 1) + 3 + NZ - 2], r_.rs_s.at[0])
    sent(r_.hs, r_.hal_s.at[0])
    sent(r_.hx, r_.hx_s.at[0])
    act_copy.wait()
    in_copy.wait()


def finish_kernel(act_h, gin_h, *refs):
    n = len(GROUPS)
    held, (ggain_h, gshift_h), refs = refs[:n], refs[n : n + 2], refs[n + 2 :]
    act_o, gin_o, proj_o, edge_o, qkv_o, out_o, up_o, down_o, ggain_o, gshift_o = refs[:10]
    summed, refs = refs[10 : 10 + n], refs[10 + n :]
    act, gin, proj, edge, qkv, out, up, down, in_sem, out_sem = refs
    loads = [
        pltpu.make_async_copy(src, dst, in_sem.at[i])
        for i, (src, dst) in enumerate(zip(held + (act_h, gin_h), summed + (act, gin), strict=True))
    ]
    for load in loads:
        load.start()
    ggain_o[...] = ggain_h[...]
    gshift_o[...] = gshift_h[...]
    stores = []

    def store(src, dst):
        copy = pltpu.make_async_copy(src, dst, out_sem.at[len(stores)])
        copy.start()
        stores.append(copy)

    def widen(dst, l, g, at, first=0, last=None):
        rows = dst.shape[1]
        for c in range(first, dst.shape[2] // 128 if last is None else last):
            dst[l, :, 128 * c : 128 * (c + 1)] = summed[g][at : at + rows].astype(F32)
            at += rows
        return at

    for g, (name, l, first, rows, _) in enumerate(GROUPS):
        loads[g].wait()
        if name == "early":
            at = widen(out, l, g, 0)
            store(out.at[l], out_o.at[l])
            at = widen(up, l, g, at)
            store(up.at[l], up_o.at[l])
            widen(down, l, g, at)
            store(down.at[l], down_o.at[l])
        elif name == "conv":
            at = widen(proj, l, g, 0)
            store(proj.at[l], proj_o.at[l])
            widen(edge, l, g, at)
            store(edge.at[l], edge_o.at[l])
        else:
            widen(qkv, l, g, 0, first // 256, (first + rows) // 256)
            if first + rows == 1536:
                store(qkv.at[l], qkv_o.at[l])
    for i, (src, dst) in enumerate(((act, act_o), (gin, gin_o))):
        loads[n + i].wait()
        store(src, dst)
    for copy in stores:
        copy.wait()


def fused_device(
    N, M, node_input, edge_feat, graph_ids, edge_src, edge_dst, halo_send, w_proj, w_edge, w_qkv,
    w_out, w_up, w_down, norm_gain, norm_shift, cotangent,
):
    R, D = node_input.shape
    E = edge_feat.shape[0]
    L = w_proj.shape[0]
    names = scratch_list(N, M, L, R, E)
    vmem = pl.BlockSpec(memory_space=pltpu.VMEM)
    hbm = pl.BlockSpec(memory_space=pltpu.HBM)
    shape = jax.ShapeDtypeStruct
    rows = shape((R, D), F32)
    norm = shape((3, L, D), F32)
    groups = [shape((rows_g, 128), BF16) for _, _, _, rows_g, _ in GROUPS]
    outs = pl.pallas_call(
        functools.partial(kernel, N, M, L, tuple(names)),
        out_shape=[rows, rows, *groups, norm, norm],
        in_specs=[hbm] + [vmem] * 4 + [hbm] * 7 + [vmem] * 2 + [hbm],
        out_specs=[hbm] * (2 + len(GROUPS)) + [vmem] * 2,
        scratch_shapes=list(names.values()),
        compiler_params=pltpu.CompilerParams(
            collective_id=0, has_side_effects=True, vmem_limit_bytes=60 << 20
        ),
        name="layers",
    )(node_input, graph_ids, edge_src, edge_dst, halo_send, edge_feat, w_proj, w_edge, w_qkv, w_out, w_up,
      w_down, norm_gain.transpose(1, 0, 2), norm_shift.transpose(1, 0, 2), cotangent)
    weights = [shape(w.shape, F32) for w in (w_proj, w_edge, w_qkv, w_out, w_up, w_down)]
    results = pl.pallas_call(
        finish_kernel,
        out_shape=[rows, rows, *weights, norm, norm],
        in_specs=[hbm] * (2 + len(GROUPS)) + [vmem] * 2,
        out_specs=[hbm] * 8 + [vmem] * 2,
        scratch_shapes=[pltpu.VMEM(s.shape, s.dtype) for s in (*groups, rows, rows, *weights)]
        + [pltpu.SemaphoreType.DMA((len(GROUPS) + 2,)), pltpu.SemaphoreType.DMA((14,))],
        compiler_params=pltpu.CompilerParams(vmem_limit_bytes=60 << 20),
        name="gradients",
    )(*outs)
    ggain, gshift = results[8].transpose(1, 0, 2), results[9].transpose(1, 0, 2)
    return (*results[:8], ggain, gshift)


BLOCK_CAP = 2048


def extended_2(block, sides, width):
    for axis, dim in sides:
        count = lax.axis_size(axis)
        forward = [(i, i + 1) for i in range(count - 1)]
        forward.append((count - 1, 0))
        backward = [(target, source) for source, target in forward]
        low = lax.ppermute(
            lax.slice_in_dim(block, block.shape[dim] - width, None, axis=dim), axis, forward
        )
        high = lax.ppermute(lax.slice_in_dim(block, 0, width, axis=dim), axis, backward)
        block = jnp.concatenate([low, block, high], axis=dim)
    return block


def block_length(total_rows, upper_limit):
    for length in range(min(total_rows, upper_limit), 0, -1):
        if total_rows % length == 0:
            return length
    return 1


def outer_product(left, right):
    return lax.dot_general(
        left, right, (((0,), (0,)), ((), ())), preferred_element_type=jnp.float32
    )


def times_transposed(left, weight):
    return lax.dot_general(
        left, weight, (((1,), (1,)), ((), ())), preferred_element_type=jnp.float32
    )


def forward_product(left, weight):
    return jnp.dot(left, weight, preferred_element_type=jnp.float32)


def silu_slope_plain(inputs):
    logistic = jax.nn.sigmoid(inputs)
    return logistic * (1.0 + inputs * (1.0 - logistic))


def normalize(inputs, gain_row, shift_row, node_total):
    batch_mean = lax.psum(jnp.sum(inputs, 0), ("nodes", "rep")) / node_total
    centred = inputs - batch_mean
    batch_var = lax.psum(jnp.sum(centred * centred, 0), ("nodes", "rep")) / node_total
    inv_std = lax.rsqrt(batch_var + NORM_EPS)
    standard = (inputs - batch_mean) * inv_std
    return (standard * gain_row + shift_row, standard, inv_std)


def normalize_back(grad_out, standard, inv_std, gain_row, node_total):
    shift_grad, gain_grad = lax.psum(
        (jnp.sum(grad_out, 0), jnp.sum(grad_out * standard, 0)), ("nodes", "rep")
    )
    grad_in = (
        gain_row
        * inv_std
        * (grad_out - shift_grad / node_total - standard * gain_grad / node_total)
    )
    return (grad_in, gain_grad, shift_grad)


def exchange_sources(outgoing):
    halo_rows = outgoing.shape[0] // 2
    grown = extended_2(outgoing, (("nodes", 0),), halo_rows)
    return jnp.concatenate([grown[:halo_rows], grown[3 * halo_rows :]], 0)


def return_sources(incoming_grad):
    halo_rows = incoming_grad.shape[0] // 2
    grown = extended_2(incoming_grad.astype(jnp.bfloat16), (("nodes", 0),), halo_rows).astype(
        incoming_grad.dtype
    )
    return jnp.concatenate([grown[:halo_rows], grown[3 * halo_rows :]], 0)


def attend_forward(query_rows, key_rows, value_rows, local_graphs, group_graphs):
    row_count = query_rows.shape[0]
    score_scale = HEAD_DIM ** (-0.5)
    queries = query_rows.reshape(row_count, HEADS, HEAD_DIM)

    def add_piece(carried, kv_piece, first_row):
        key_piece, value_piece = kv_piece
        piece_rows = key_piece.shape[0]
        block_len = block_length(piece_rows, BLOCK_CAP)

        def add_block(block_state, block_index):
            row_max, row_sum, accumulated = block_state
            block_start = block_index * block_len
            key_block = lax.dynamic_slice_in_dim(key_piece, block_start, block_len, 0).reshape(
                block_len, HEADS, HEAD_DIM
            )
            value_block = lax.dynamic_slice_in_dim(value_piece, block_start, block_len, 0).reshape(
                block_len, HEADS, HEAD_DIM
            )
            key_graphs = lax.dynamic_slice_in_dim(
                group_graphs, first_row + block_start, block_len, 0
            )
            same_graph = (local_graphs[:, None] == key_graphs[None, :])[None]
            scores = (
                jnp.einsum("qhd,khd->hqk", queries, key_block, preferred_element_type=jnp.float32)
                * score_scale
            )
            scores = jnp.where(same_graph, scores, NEG)
            new_max = jnp.maximum(row_max, jnp.max(scores, 2))
            weights = jnp.where(same_graph, jnp.exp(scores - new_max[:, :, None]), 0.0)
            factor = jnp.exp(row_max - new_max)
            row_sum = row_sum * factor + jnp.sum(weights, 2)
            contrib = jnp.einsum(
                "hqk,khd->qhd",
                weights.astype(jnp.bfloat16),
                value_block,
                preferred_element_type=jnp.float32,
            )
            accumulated = accumulated * jnp.transpose(factor)[:, :, None] + contrib
            return ((new_max, row_sum, accumulated), None)

        carried, _ = lax.scan(add_block, carried, jnp.arange(piece_rows // block_len))
        return carried

    start_state = (
        jnp.full((HEADS, row_count), NEG, jnp.float32),
        jnp.zeros((HEADS, row_count), jnp.float32),
        jnp.zeros((row_count, HEADS, HEAD_DIM), jnp.float32),
    )
    row_max, row_sum, accumulated = add_piece(
        start_state,
        (
            lax.all_gather(key_rows, "nodes", axis=0, tiled=True),
            lax.all_gather(value_rows, "nodes", axis=0, tiled=True),
        ),
        jnp.int32(0),
    )
    attn_raw = accumulated / jnp.transpose(row_sum)[:, :, None]
    log_sum = row_max + jnp.log(row_sum)
    return (attn_raw, log_sum)


def attend_backward(
    query_rows, key_rows, value_rows, grad_low, attn_raw, log_sum, local_graphs, group_graphs
):
    row_count = query_rows.shape[0]
    model_width = HEADS * HEAD_DIM
    score_scale = HEAD_DIM ** (-0.5)
    queries = query_rows.reshape(row_count, HEADS, HEAD_DIM)
    grad_heads = grad_low.reshape(row_count, HEADS, HEAD_DIM)
    row_delta = jnp.einsum("qhd,qhd->hq", grad_heads.astype(jnp.float32), attn_raw)

    def score_block(key_block, value_block, key_graphs):
        same_graph = (local_graphs[:, None] == key_graphs[None, :])[None]
        scores = (
            jnp.einsum("qhd,khd->hqk", queries, key_block, preferred_element_type=jnp.float32)
            * score_scale
        )
        attn_weights = jnp.exp(jnp.where(same_graph, scores - log_sum[:, :, None], NEG))
        grad_weights = jnp.einsum(
            "qhd,khd->hqk", grad_heads, value_block, preferred_element_type=jnp.float32
        )
        grad_scores = (attn_weights * (grad_weights - row_delta[:, :, None])).astype(jnp.bfloat16)
        return (attn_weights, grad_scores)

    def key_terms(attn_weights, grad_scores, block_len):
        grad_keys = (
            jnp.einsum("hqk,qhd->khd", grad_scores, queries, preferred_element_type=jnp.float32)
            * score_scale
        )
        grad_values = jnp.einsum(
            "hqk,qhd->khd",
            attn_weights.astype(jnp.bfloat16),
            grad_heads,
            preferred_element_type=jnp.float32,
        )
        return jnp.concatenate(
            [
                grad_keys.reshape(block_len, model_width),
                grad_values.reshape(block_len, model_width),
            ],
            1,
        )

    def query_term(grad_scores, key_block):
        return (
            jnp.einsum("hqk,khd->qhd", grad_scores, key_block, preferred_element_type=jnp.float32)
            * score_scale
        )

    group_rows = group_graphs.shape[0]

    def add_piece(carried, kv_piece, first_row):
        key_piece, value_piece = kv_piece
        piece_rows = key_piece.shape[0]
        block_len = block_length(piece_rows, BLOCK_CAP)

        def add_block(block_state, block_index):
            grad_query, buffer = block_state
            block_start = block_index * block_len
            key_block = lax.dynamic_slice_in_dim(key_piece, block_start, block_len, 0).reshape(
                block_len, HEADS, HEAD_DIM
            )
            value_block = lax.dynamic_slice_in_dim(value_piece, block_start, block_len, 0).reshape(
                block_len, HEADS, HEAD_DIM
            )
            place = first_row + block_start
            key_graphs = lax.dynamic_slice_in_dim(group_graphs, place, block_len, 0)
            attn_weights, grad_scores = score_block(key_block, value_block, key_graphs)
            grad_query = grad_query + query_term(grad_scores, key_block)
            block_terms = key_terms(attn_weights, grad_scores, block_len)
            current = lax.dynamic_slice_in_dim(buffer, place, block_len, 0)
            buffer = lax.dynamic_update_slice_in_dim(buffer, current + block_terms, place, 0)
            return ((grad_query, buffer), None)

        carried, _ = lax.scan(add_block, carried, jnp.arange(piece_rows // block_len))
        return carried

    start_state = (
        jnp.zeros((row_count, HEADS, HEAD_DIM), jnp.float32),
        jnp.zeros((group_rows, 2 * model_width), jnp.float32),
    )
    grad_query, buffer = add_piece(
        start_state,
        (
            lax.all_gather(key_rows, "nodes", axis=0, tiled=True),
            lax.all_gather(value_rows, "nodes", axis=0, tiled=True),
        ),
        jnp.int32(0),
    )
    grad_kv = lax.psum_scatter(buffer, "nodes", scatter_dimension=0, tiled=True)
    return (
        grad_query.reshape(row_count, model_width),
        grad_kv[:, :model_width],
        grad_kv[:, model_width:],
    )


def layer_forward(
    hidden, params, edge_feat, edge_src, edge_dst, halo_send, local_graphs, group_graphs, node_total
):
    w_proj, w_edge, w_qkv, w_out, w_up, w_down, norm_gains, norm_shifts = params
    row_count, model_width = hidden.shape
    hidden_low = hidden.astype(jnp.bfloat16)
    projected = forward_product(hidden_low, w_proj)
    self_term = projected[:, :model_width]
    dest_term = projected[:, 2 * model_width : 3 * model_width]
    source_rows = jnp.concatenate(
        [projected[:, model_width : 2 * model_width], projected[:, 3 * model_width :]], 1
    ).astype(jnp.bfloat16)
    incoming = exchange_sources(source_rows[halo_send])
    extended = jnp.concatenate([source_rows, incoming], 0)
    edge_rows = extended[edge_src].astype(jnp.float32)
    source_b = edge_rows[:, :model_width]
    source_e = edge_rows[:, model_width:]
    edge_proj = forward_product(edge_feat, w_edge)
    gating = jax.nn.sigmoid(dest_term[edge_dst] + source_e + edge_proj)
    numerator = jax.ops.segment_sum(gating * source_b, edge_dst, row_count)
    denominator = jax.ops.segment_sum(gating, edge_dst, row_count)
    message = self_term + numerator / (denominator + GATE_EPS)
    normed_one, standard_one, inv_one = normalize(
        message, norm_gains[0], norm_shifts[0], node_total
    )
    local_out = hidden + jax.nn.silu(normed_one)
    qkv_low = forward_product(hidden_low, w_qkv).astype(jnp.bfloat16)
    query_rows = qkv_low[:, :model_width]
    key_rows = qkv_low[:, model_width : 2 * model_width]
    value_rows = qkv_low[:, 2 * model_width :]
    attn_raw, log_sum = attend_forward(query_rows, key_rows, value_rows, local_graphs, group_graphs)
    attn_low = attn_raw.reshape(row_count, model_width).astype(jnp.bfloat16)
    attn_proj = forward_product(attn_low, w_out)
    normed_two, standard_two, inv_two = normalize(
        hidden + attn_proj, norm_gains[1], norm_shifts[1], node_total
    )
    mixed = local_out + normed_two
    mixed_low = mixed.astype(jnp.bfloat16)
    up_proj = forward_product(mixed_low, w_up)
    activated = jax.nn.silu(up_proj).astype(jnp.bfloat16)
    down_proj = forward_product(activated, w_down)
    normed_three, standard_three, inv_three = normalize(
        mixed + down_proj, norm_gains[2], norm_shifts[2], node_total
    )
    saved = (
        hidden_low,
        source_b,
        gating,
        numerator,
        denominator,
        normed_one,
        standard_one,
        inv_one,
        query_rows,
        key_rows,
        value_rows,
        attn_raw,
        log_sum,
        attn_low,
        standard_two,
        inv_two,
        mixed_low,
        up_proj,
        activated,
        standard_three,
        inv_three,
    )
    return (normed_three, saved)


def layer_backward(
    grad_out,
    params,
    saved,
    edge_feat,
    edge_src,
    edge_dst,
    halo_send,
    local_graphs,
    group_graphs,
    node_total,
):
    w_proj, w_edge, w_qkv, w_out, w_up, w_down, norm_gains, norm_shifts = params
    (
        hidden_low,
        source_b,
        gating,
        numerator,
        denominator,
        normed_one,
        standard_one,
        inv_one,
        query_rows,
        key_rows,
        value_rows,
        attn_raw,
        log_sum,
        attn_low,
        standard_two,
        inv_two,
        mixed_low,
        up_proj,
        activated,
        standard_three,
        inv_three,
    ) = saved
    row_count, model_width = grad_out.shape
    grad_three, gain_three, shift_three = normalize_back(
        grad_out, standard_three, inv_three, norm_gains[2], node_total
    )
    down_grad = grad_three.astype(jnp.bfloat16)
    grad_w_down = outer_product(activated, down_grad)
    up_grad = (times_transposed(down_grad, w_down) * silu_slope_plain(up_proj)).astype(jnp.bfloat16)
    grad_w_up = outer_product(mixed_low, up_grad)
    grad_mixed = grad_three + times_transposed(up_grad, w_up)
    grad_two, gain_two, shift_two = normalize_back(
        grad_mixed, standard_two, inv_two, norm_gains[1], node_total
    )
    out_grad = grad_two.astype(jnp.bfloat16)
    grad_w_out = outer_product(attn_low, out_grad)
    attn_grad = times_transposed(out_grad, w_out).astype(jnp.bfloat16)
    grad_query, grad_key, grad_value = attend_backward(
        query_rows, key_rows, value_rows, attn_grad, attn_raw, log_sum, local_graphs, group_graphs
    )
    qkv_grad = jnp.concatenate([grad_query, grad_key, grad_value], 1).astype(jnp.bfloat16)
    grad_w_qkv = outer_product(hidden_low, qkv_grad)
    grad_message, gain_one, shift_one = normalize_back(
        grad_mixed * silu_slope_plain(normed_one), standard_one, inv_one, norm_gains[0], node_total
    )
    shifted = denominator + GATE_EPS
    grad_numer = grad_message / shifted
    grad_denom = -grad_message * numerator / (shifted * shifted)
    numer_edge = grad_numer[edge_dst]
    grad_gate = numer_edge * source_b + grad_denom[edge_dst]
    grad_pre_edge = grad_gate * gating * (1.0 - gating)
    edge_grad = grad_pre_edge.astype(jnp.bfloat16)
    grad_w_edge = outer_product(edge_feat, edge_grad)
    grad_dest = jax.ops.segment_sum(grad_pre_edge, edge_dst, row_count)
    grad_extended = jax.ops.segment_sum(
        jnp.concatenate([numer_edge * gating, grad_pre_edge], 1),
        edge_src,
        row_count + halo_send.shape[0],
    )
    returned = return_sources(grad_extended[row_count:])
    grad_source = grad_extended[:row_count].at[halo_send].add(returned)
    proj_grad = jnp.concatenate(
        [grad_message, grad_source[:, :model_width], grad_dest, grad_source[:, model_width:]], 1
    ).astype(jnp.bfloat16)
    grad_w_proj = outer_product(hidden_low, proj_grad)
    grad_hidden = (
        grad_mixed
        + grad_two
        + times_transposed(proj_grad, w_proj)
        + times_transposed(qkv_grad, w_qkv)
    )
    weight_grads = (grad_w_proj, grad_w_edge, grad_w_qkv, grad_w_out, grad_w_up, grad_w_down)
    return (
        grad_hidden,
        weight_grads,
        jnp.stack([gain_one, gain_two, gain_three]),
        jnp.stack([shift_one, shift_two, shift_three]),
    )


def per_device(
    node_input,
    edge_feat,
    graph_ids,
    edge_src,
    edge_dst,
    halo_send,
    w_proj,
    w_edge,
    w_qkv,
    w_out,
    w_up,
    w_down,
    norm_gain,
    norm_shift,
    cotangent,
):
    group_graphs = lax.all_gather(graph_ids, "nodes", axis=0, tiled=True)
    node_total = node_input.shape[0] * lax.axis_size("nodes") * lax.axis_size("rep")
    layer_count = w_proj.shape[0]
    layer_params = [
        (
            w_proj[layer_index],
            w_edge[layer_index],
            w_qkv[layer_index],
            w_out[layer_index],
            w_up[layer_index],
            w_down[layer_index],
            norm_gain[layer_index],
            norm_shift[layer_index],
        )
        for layer_index in range(layer_count)
    ]
    hidden = node_input.astype(jnp.float32)
    saved_all = []
    for layer_index in range(layer_count):
        hidden, saved = layer_forward(
            hidden,
            layer_params[layer_index],
            edge_feat,
            edge_src,
            edge_dst,
            halo_send,
            graph_ids,
            group_graphs,
            node_total,
        )
        saved_all.append(saved)
    grad_hidden = cotangent.astype(jnp.float32)
    weight_parts = [None] * layer_count
    gain_parts = [None] * layer_count
    shift_parts = [None] * layer_count
    for layer_index in range(layer_count - 1, -1, -1):
        (
            grad_hidden,
            weight_parts[layer_index],
            gain_parts[layer_index],
            shift_parts[layer_index],
        ) = layer_backward(
            grad_hidden,
            layer_params[layer_index],
            saved_all[layer_index],
            edge_feat,
            edge_src,
            edge_dst,
            halo_send,
            graph_ids,
            group_graphs,
            node_total,
        )
    proj_local = jnp.stack([weight_parts[layer_index][0] for layer_index in range(layer_count)])
    edge_local = jnp.stack([weight_parts[layer_index][1] for layer_index in range(layer_count)])
    qkv_local = jnp.stack([weight_parts[layer_index][2] for layer_index in range(layer_count)])
    out_local = jnp.stack([weight_parts[layer_index][3] for layer_index in range(layer_count)])
    up_local = jnp.stack([weight_parts[layer_index][4] for layer_index in range(layer_count)])
    down_local = jnp.stack([weight_parts[layer_index][5] for layer_index in range(layer_count)])
    grad_proj, grad_edge, grad_qkv, grad_out, grad_up, grad_down = lax.psum(
        (proj_local, edge_local, qkv_local, out_local, up_local, down_local), ("nodes", "rep")
    )
    return (
        hidden,
        grad_hidden,
        grad_proj,
        grad_edge,
        grad_qkv,
        grad_out,
        grad_up,
        grad_down,
        jnp.stack(gain_parts),
        jnp.stack(shift_parts),
    )


def solution(mesh):
    in_specs = (
        P(("rep", "nodes"), None),
        P(("rep", "nodes"), None),
        P(("rep", "nodes")),
        P(("rep", "nodes")),
        P(("rep", "nodes")),
        P(("rep", "nodes")),
        P(),
        P(),
        P(),
        P(),
        P(),
        P(),
        P(),
        P(),
        P(("rep", "nodes"), None),
    )
    out_specs = (
        P(("rep", "nodes"), None),
        P(("rep", "nodes"), None),
        P(),
        P(),
        P(),
        P(),
        P(),
        P(),
        P(),
        P(),
    )
    N, M = mesh.shape["nodes"], mesh.shape["rep"]
    fused = N in (4, 8) and M % 2 == 0 and 512 % (16 * N * M) == 0
    return jax.shard_map(
        functools.partial(fused_device, N, M) if fused else per_device,
        mesh=mesh, in_specs=in_specs, out_specs=out_specs, check_vma=False,
    )
```

```python
import functools
import math

import jax
import jax.numpy as jnp
from jax import lax
from jax.experimental import pallas as pl
from jax.experimental.pallas import tpu as pltpu
from jax.sharding import PartitionSpec as P

HEADS = 8
HEAD_DIM = 32
NEG = -1e30
NORM_EPS = 1e-05
GATE_EPS = 1e-06
F32, BF16, I32 = jnp.float32, jnp.bfloat16, jnp.int32
MESH = pl.DeviceIdType.MESH
SYNCS = 12
STRIP = 32
GROUPS = (
    ("early", 1, 0, 2560, ("core", "y", "x", "z")),
    ("conv", 1, 0, 2560, ("core", "y", "x", "z")),
    ("qkv", 1, 0, 1536, ("core", "y", "x", "z")),
    ("early", 0, 0, 2560, ("core", "x", "y", "z")),
    ("conv", 0, 0, 2560, ("core", "y", "x", "z")),
    ("qkv", 0, 0, 1024, ("rep", "nodes")),
    ("qkv", 0, 1024, 512, ("nodes", "rep")),
)


def dot(left, right):
    return lax.dot_general(
        left, right, (((1,), (0,)), ((), ())), preferred_element_type=F32
    )


def dot_nt(left, right):
    return lax.dot_general(
        left, right, (((1,), (1,)), ((), ())), preferred_element_type=F32
    )


def dot_tn(left, right):
    return lax.dot_general(
        left, right, (((0,), (0,)), ((), ())), preferred_element_type=F32
    )


def split(value):
    high = value.astype(BF16)
    return high, (value - high.astype(F32)).astype(BF16)


def sigmoid(value):
    return jax.nn.sigmoid(value)


def silu_slope(value):
    logistic = sigmoid(value)
    return logistic * (1.0 + value * (1.0 - logistic))


def col_sum(value):
    return jnp.sum(value, axis=0, keepdims=True)


def pack(first, second):
    return jnp.concatenate([first[:, :128], first[:, 128:], second[:, :128], second[:, 128:]], 0)


def unpack(tile):
    return [jnp.concatenate([tile[i : i + 1], tile[i + 1 : i + 2]], 1) for i in (0, 2)]


def combine_moments(tiles, count):
    mean = jnp.mean(tiles[:, 0:2], 0)
    off = tiles[:, 0:2] - mean
    return jnp.concatenate([mean, jnp.sum(tiles[:, 2:4] + count * off * off, 0)], 0)


class Refs:
    pass


def axis_sizes(N, M):
    return dict(core=2, y=M // 2, x=2, z=N // 2, rep=M, nodes=N)


def scratch_list(N, M, L, R, E):
    NZ, NB, G = N // 2, N // 4, N * R
    D, FF, W, HH = 256, 512, 4 * R, HEADS // 2 * R
    dma = lambda *shape: pltpu.SemaphoreType.DMA(shape)
    vm = lambda dtype, *shape: pltpu.VMEM(shape, dtype)
    names = dict(
        gb=vm(BF16, L, N, R, D),
        xs=vm(BF16, L, N, R, D),
        meta=vm(I32, N, 8, 256),
        cot=vm(BF16, R, D),
        wp=vm(BF16, L, D, 4 * D),
        we=vm(BF16, L, D, D),
        wqkv=vm(BF16, L, D, 3 * D),
        wo=vm(BF16, L, D, D),
        wu=vm(BF16, L, D, FF),
        wd=vm(BF16, L, FF, D),
        st1=vm(F32, SYNCS, M * N, 4, 128),
        gain=vm(F32, L, 8, D),
        shift=vm(F32, L, 8, D),
        ggain=vm(F32, L, 8, D),
        gshift=vm(F32, L, 8, D),
        iv=vm(F32, L, 8, D),
        moff=vm(F32, N, 8, D),
        move=vm(F32, 8, D),
        le=vm(BF16, E, 1024),
        re=vm(BF16, 1024, D),
        TT=vm(BF16, R, 2 * E),
        ST=vm(BF16, 256, E),
        efT=vm(BF16, D, E),
        HS=vm(BF16, 64, R),
        hx=vm(BF16, L, 64, D),
        A=vm(BF16, R, 64),
        bias=vm(F32, R, G),
        xf=vm(F32, L + 1, R, D),
        xe=vm(BF16, L, 256, D),
        xeT=vm(BF16, D, 256),
        gate=vm(F32, L, E, D),
        bs=vm(BF16, L, E, D),
        num=vm(F32, L, R, D),
        den=vm(F32, L, R, D),
        z0=vm(F32, L, R, D),
        z1=vm(F32, L, R, D),
        z2=vm(F32, L, R, D),
        wkvT=vm(BF16, L, 2 * D, D),
        kvT=vm(BF16, L, 2 * D, G),
        odT=vm(F32, NB, D, R),
        ldT=vm(F32, NB, D, R),
        md=vm(F32, NB, R, D),
        rb=vm(F32, L, NB, R, D),
        pst=vm(BF16, L, HEADS * R, G),
        oraw=vm(F32, L, R, D),
        ob=vm(BF16, L, R, D),
        mb=vm(BF16, L, R, D),
        u=vm(F32, L, R, FF),
        g=vm(BF16, L, R, FF),
        dy=vm(F32, R, D),
        dmix=vm(F32, R, D),
        gy0=vm(F32, R, D),
        local=vm(F32, R, D),
        dxo=vm(F32, R, D),
        dob=vm(F32, R, D),
        dqT=vm(F32, D, R),
        qm=vm(BF16, L, 2, HH, 128),
        q=vm(BF16, L, R, D),
        qT=vm(BF16, D, R),
        dosT=vm(BF16, 128, R),
        dom=vm(BF16, HH, 256),
        sc=vm(F32, 2, max(2 * R, E), W),
        tp=vm(F32, HEADS // 2, R, 128),
        dss=vm(BF16, HH, W),
        dkv=vm(BF16, 2 * D, W),
        gkv=vm(F32, 2 * D, D),
        gg=vm(BF16, 2 * E, 2 * D),
        dn=vm(BF16, 512, 2 * D),
        dproj=vm(BF16, 256, 4 * D),
        dxs=vm(BF16, L, NZ, 2, R, D),
        rs1=vm(BF16, L, NZ, R, D),
        cs=vm(BF16, L, NZ, R, D),
        rs2=vm(BF16, L, NZ, R, D),
        ro=vm(BF16, L, 3, R, D),
        hs=vm(BF16, L, 2, 32, D),
        hr=vm(BF16, L, 2, 32, D),
    )
    names.update(
        gs_early=vm(BF16, L, 2560, 128),
        gs_conv=vm(BF16, L, 2560, 128),
        gs_qkv=vm(BF16, L, 1536, 128),
    )
    sizes = axis_sizes(N, M)
    for g, (_, _, _, rows, stages) in enumerate(GROUPS):
        names[f"go{g}"] = vm(BF16, rows, 128)
        left = rows
        for k, axis in enumerate(stages):
            left //= sizes[axis]
            names[f"ga{g}_{k}"] = vm(BF16, sizes[axis] - 1, left, 128)
            if k < len(stages) - 1:
                names[f"gh{g}_{k}"] = vm(BF16, left, 128)
    names.update(
        ar_s=dma(len(GROUPS)),
        ar_r=dma(sum(2 * len(stages) for *_, stages in GROUPS)),
        ar_l=dma(len(GROUPS)),
        load=dma(9),
        store=dma(2),
        meta_s=dma(1),
        meta_r=dma(1),
        st_s=dma(1),
        st_r=dma(SYNCS),
        ag_s=dma(1),
        agn_r=dma(L),
        agc_r=dma(L, NZ),
        agp_r=dma(L),
        rs_s=dma(1),
        rsp_r=dma(L, NB, 2),
        ro_r=dma(L),
        rsc_r=dma(L),
        hx_s=dma(1),
        hx_r=dma(L),
        hal_s=dma(1),
        hal_r=dma(L),
    )
    return names


IN_NAMES = (
    "x_in", "ids", "edge_src", "edge_dst", "halo", "ef_h", "wp_h", "we_h", "wqkv_h", "wo_h", "wu_h", "wd_h",
    "gain_in", "shift_in", "cot_h",
)
OUT_NAMES = ("out_act", "grad_in", *(f"gout{g}" for g in range(len(GROUPS))), "ggain_out", "gshift_out")


def kernel(N, M, L, names, *args):
    r_ = Refs()
    for name, ref in zip(IN_NAMES + OUT_NAMES + tuple(names), args, strict=True):
        setattr(r_, name, ref)
    R, D = r_.x_in.shape
    E = r_.ef_h.shape[0]
    NZ, NB, G, W = N // 2, N // 4, N * R, 4 * R
    HK = HEADS // 2
    total = float(N * M * R)
    scale = HEAD_DIM ** -0.5
    me = lax.axis_index("nodes")
    rep = lax.axis_index("rep")
    z = me // 2
    par = me % 2
    partner = 2 * z + (1 - par)
    prev = (me + N - 1) % N
    nxt = (me + 1) % N
    zh, zl = z // 2, z % 2
    z_to = lambda t: 2 * ((zh + t // 2) % NB) + (zl + t % 2) % 2
    z_from = lambda t: 2 * ((zh + NB - t // 2) % NB) + (zl + t % 2) % 2

    def remote(src, dst, s_sem, r_sem, **where):
        return pltpu.make_async_remote_copy(
            src_ref=src, dst_ref=dst, send_sem=s_sem, recv_sem=r_sem,
            device_id=where, device_id_type=MESH,
        )

    def send(src, dst, s_sem, r_sem, **where):
        remote(src, dst, s_sem, r_sem, **where).start()

    def send_rows(src, dst, rows, s_sem, r_sem, **where):
        pieces = next(p for p in range(1, rows) if rows % (16 * p) == 0 and rows // p <= 128)
        for at in range(0, rows, rows // pieces):
            cut = pl.ds(at, rows // pieces)
            send(src.at[cut], dst.at[cut], s_sem, r_sem, **where)

    def arrive(dst, r_sem):
        remote(dst, dst, r_sem, r_sem, nodes=partner).wait_recv()

    def sent(src, s_sem):
        remote(src, src, s_sem, s_sem, nodes=partner).wait_send()

    def when(condition, *acts):
        if condition:
            for act in acts:
                act()

    loads = [pltpu.make_async_copy(r_.ef_h, r_.le.at[:, D : 2 * D], r_.load.at[0])] + [
        pltpu.make_async_copy(getattr(r_, f"{name}_h"), getattr(r_, name), r_.load.at[1 + i])
        for i, name in enumerate(("we", "wqkv", "wp", "wo", "wu", "wd", "cot"))
    ]
    own_rows = pltpu.make_async_copy(r_.x_in, r_.gb.at[0, me], r_.load.at[8])
    own_rows.start()
    for load in loads:
        load.start()

    barrier = pltpu.get_barrier_semaphore()
    for dr in range(M):
        for d in range(N):
            if dr + d > 0:
                pl.semaphore_signal(barrier, inc=1, device_id={"rep": (rep + dr) % M, "nodes": (me + d) % N},
                                    device_id_type=MESH)
    pl.semaphore_wait(barrier, M * N - 1)

    def gather_start(l):
        mine = r_.gb.at[l, me]
        for t in range(2, NZ):
            send_rows(mine, mine, R, r_.ag_s.at[0], r_.agc_r.at[l, t], nodes=2 * z_to(t) + par)
        send_rows(mine, mine, R, r_.ag_s.at[0], r_.agn_r.at[l], nodes=partner)
        send_rows(mine, mine, R, r_.ag_s.at[0], r_.agn_r.at[l], nodes=2 * z_to(1) + par)
        send_rows(mine, mine, R, r_.ag_s.at[0], r_.agn_r.at[l], nodes=2 * z_to(1) + 1 - par)

    def gather_pass(l, t):
        piece = r_.gb.at[l, 2 * z_from(t) + par]
        arrive(piece, r_.agc_r.at[l, t])
        send_rows(piece, piece, R, r_.ag_s.at[0], r_.agp_r.at[l], nodes=partner)

    def gather_near(l):
        arrive(r_.gb.at[l, 0:3], r_.agn_r.at[l])

    def gather_far(l):
        arrive(r_.gb.at[l, 0 : NZ - 2], r_.agp_r.at[l])

    def sync_start(k, first, second):
        mine = rep * N + me
        r_.st1[k, mine] = pack(first, second)
        for dr in range(M):
            for d in range(N):
                if dr + d > 0:
                    send(r_.st1.at[k, mine], r_.st1.at[k, mine], r_.st_s.at[0], r_.st_r.at[k],
                         rep=(rep + dr) % M, nodes=(me + d) % N)

    def sync_wait(k):
        arrive(r_.st1.at[k, 0 : M * N - 1], r_.st_r.at[k])

    def sync_moments(k):
        sync_wait(k)
        return unpack(combine_moments(r_.st1[k], float(R)))

    def sync_sums(k):
        sync_wait(k)
        return unpack(jnp.sum(r_.st1[k], 0))

    sizes = axis_sizes(N, M)
    core, row = rep % 2, rep // 2
    places = dict(
        core=(core, lambda t: dict(rep=2 * row + t)),
        y=(row, lambda t: dict(rep=2 * t + core)),
        x=(par, lambda t: dict(nodes=2 * z + t)),
        z=(z, lambda t: dict(nodes=2 * t + par)),
        rep=(rep, lambda t: dict(rep=t)),
        nodes=(me, lambda t: dict(nodes=t)),
    )

    def reduce_step(g, step):
        name, layer, first, rows, stages = GROUPS[g]
        K = len(stages)
        base = sum(2 * len(before) for *_, before in GROUPS[:g])
        gs, out = getattr(r_, f"gs_{name}").at[layer, first : first + rows], getattr(r_, f"go{g}")
        count, offset = [rows], [0]
        for axis in stages:
            count.append(count[-1] // sizes[axis])
            offset.append(offset[-1] + places[axis][0] * count[-1])
        take = lambda start, size: pl.ds(pl.multiple_of(start, 16), size)
        if 1 <= step <= K:
            k = step - 1
            got = getattr(r_, f"ga{g}_{k}")
            arrive(got, r_.ar_r.at[base + k])
            held = gs if k == 0 else getattr(r_, f"gh{g}_{k - 1}")
            index = places[stages[k]][0]
            acc = held[take(index * count[k + 1], count[k + 1])].astype(F32)
            for slot in range(sizes[stages[k]] - 1):
                acc = acc + got[slot].astype(F32)
            if step < K:
                getattr(r_, f"gh{g}_{k}")[...] = acc.astype(BF16)
            else:
                out[take(offset[K], count[K])] = acc.astype(BF16)
        elif step > K:
            k = 2 * K - step
            arrive(out.at[0 : (sizes[stages[k]] - 1) * count[k + 1]], r_.ar_r.at[base + step - 1])
        if step < K:
            held = gs if step == 0 else getattr(r_, f"gh{g}_{step - 1}")
            index, device = places[stages[step]]
            size = sizes[stages[step]]
            for d in range(1, size):
                to = (index + d) % size
                send_rows(held.at[take(to * count[step + 1], count[step + 1])], getattr(r_, f"ga{g}_{step}").at[d - 1],
                     count[step + 1], r_.ar_s.at[g], r_.ar_r.at[base + step], **device(to))
        elif step < 2 * K:
            k = 2 * K - 1 - step
            index, device = places[stages[k]]
            size = sizes[stages[k]]
            here = out.at[take(offset[k + 1], count[k + 1])]
            for d in range(1, size):
                send_rows(here, here, count[k + 1], r_.ar_s.at[g], r_.ar_r.at[base + step],
                          **device((index + d) % size))
        else:
            pltpu.make_async_copy(out, getattr(r_, f"gout{g}"), r_.ar_l.at[g]).start()

    def reduce_drain(g):
        name, _, _, rows, _ = GROUPS[g]
        sent(getattr(r_, f"gs_{name}").at[:, 0 : rows - rows // (M * N)], r_.ar_s.at[g])
        pltpu.make_async_copy(getattr(r_, f"go{g}"), getattr(r_, f"gout{g}"), r_.ar_l.at[g]).wait()

    def put(buf, l, at, value):
        rows = value.shape[0]
        for c in range(value.shape[1] // 128):
            buf[l, at : at + rows] = value[:, 128 * c : 128 * (c + 1)].astype(BF16)
            at += rows
        return at

    lane_head = lax.broadcasted_iota(I32, (R, 128), 1) // HEAD_DIM

    def by_head(parts):
        out = parts[0]
        for k in range(1, HK):
            out = jnp.where(lane_head == k, parts[k], out)
        return out

    r_.meta[me] = jnp.full((8, 256), -1, I32)
    r_.meta[me, 0:1, 0:R] = r_.ids[...].reshape(1, R)
    r_.meta[me, 1:2, 0:48] = r_.halo[...].reshape(1, 48)
    for d in range(1, N):
        send(r_.meta.at[me], r_.meta.at[me], r_.meta_s.at[0], r_.meta_r.at[0], nodes=(me + d) % N)
    own_rows.wait()
    gather_start(0)

    src_row = r_.edge_src[...].reshape(1, E)
    src_row = jnp.where(src_row < R + 24, src_row, src_row + 8)
    dst_row = r_.edge_dst[...].reshape(1, E)
    src_col = jnp.broadcast_to(src_row, (128, E)).T[:, 0:1]
    dst_col = jnp.broadcast_to(dst_row, (128, E)).T[:, 0:1]
    as_mask = lambda cond: cond.astype(F32).astype(BF16)
    r_.le[:, 0:256] = as_mask(src_col == lax.broadcasted_iota(I32, (E, 256), 1))
    target = as_mask(dst_col == lax.broadcasted_iota(I32, (E, 256), 1))
    r_.le[:, 512:768] = target
    r_.le[:, 768:1024] = target
    target = as_mask(dst_row == lax.broadcasted_iota(I32, (R, E), 0))
    r_.TT[:, 0:E] = target
    r_.TT[:, E:] = target
    r_.ST[...] = as_mask(src_row == lax.broadcasted_iota(I32, (256, E), 0))
    r_.dn[R:256] = jnp.zeros((256 - R, 2 * D), BF16)
    r_.dn[256 + R : 512] = jnp.zeros((256 - R, 2 * D), BF16)
    r_.dproj[R:256, 0:D] = jnp.zeros((256 - R, D), BF16)
    r_.dproj[R:256, 2 * D : 3 * D] = jnp.zeros((256 - R, D), BF16)
    halo_col = jnp.broadcast_to(r_.meta[me][1:2, 0:128], (128, 128)).T
    hot = (halo_col[0:48, 0:1] == lax.broadcasted_iota(I32, (48, R), 1)).astype(F32)
    pad = jnp.zeros((8, R), F32)
    r_.HS[...] = jnp.concatenate([hot[0:24], pad, hot[24:48], pad], 0).astype(BF16)
    loads[0].wait()
    r_.efT[...] = r_.le[:, D : 2 * D].T
    for l in range(L):
        for k in range(3):
            r_.gain[l, k : k + 1] = r_.gain_in[k, l : l + 1]
            r_.shift[l, k : k + 1] = r_.shift_in[k, l : l + 1]
    r_.xf[0] = r_.gb[0, me].astype(F32)
    r_.moff[...] = jnp.zeros((N, 8, D), F32)
    r_.move[0:1] = jnp.ones((1, D), F32)
    r_.move[1:2] = jnp.zeros((1, D), F32)
    for load in loads[1:]:
        load.wait()
    for l in range(L):
        r_.wkvT[l] = r_.wqkv[l, :, D:].T

    arrive(r_.meta.at[0 : N - 1], r_.meta_r.at[0])
    id_col = jnp.broadcast_to(r_.meta[me][0:1, 0:R], (128, R)).T[:, 0:1]
    id_row = jnp.concatenate(
        [r_.meta[4 * ((zh + NB - j // 4) % NB) + j % 4][0:1, 0:R] for j in range(N)], 1
    )
    r_.bias[...] = jnp.where(id_col == id_row, 0.0, NEG)

    r_.A[...] = as_mask(r_.meta[me][1:2, 0:64] == lax.broadcasted_iota(I32, (R, 64), 0))

    factor_exp = scale * math.log2(math.e)

    def prepare_queries(l):
        q = dot(r_.xs[l, me], r_.wqkv[l, :, :D]).astype(BF16)
        r_.q[l] = q
        q = q.astype(F32)
        for hf in range(2):
            for k in range(HK):
                part = jnp.where(lane_head == k, q[:, 128 * hf : 128 * (hf + 1)], 0.0)
                r_.qm[l, hf, k * R : (k + 1) * R] = part.astype(BF16)

    def head_dims(hf, k, base=0):
        first = base + hf * 128 + k * HEAD_DIM
        return slice(first, first + HEAD_DIM)

    def head_rows(hf, k, count=1):
        return slice((hf * HK + k) * R, (hf * HK + k + count) * R)

    def lane_half(hf):
        return slice(hf * 128, (hf + 1) * 128)

    def half_of(i):
        return (zh + NB - i) % NB, slice(i * W, (i + 1) * W)

    def attention_keys(l, i):
        half, rows = half_of(i)
        x = r_.xs[l, pl.ds(4 * half, 4)].reshape(W, D)
        r_.kvT[l, :, rows] = dot_nt(r_.wkvT[l], x).astype(BF16)

    def attention_heads(l, i, hfs):
        _, rows = half_of(i)
        for hf in hfs:
            lanes = lane_half(hf)
            ones = jnp.ones((HEAD_DIM, W), BF16)
            for c in range(HK // 2):
                r_.sc[c % 2, 0 : 2 * R] = dot(r_.qm[l, hf, 2 * c * R : 2 * (c + 1) * R], r_.kvT[l, lanes, rows])
                for k in range(2):
                    for at in range(0, R, STRIP):
                        s = r_.sc[c % 2, k * R + at : k * R + at + STRIP] + r_.bias[at : at + STRIP, rows]
                        top = jnp.max(s, 1, keepdims=True)
                        e = jnp.exp2((s - top) * factor_exp)
                        r_.tp[2 * c + k, at : at + STRIP] = jnp.broadcast_to(top, (STRIP, 128))
                        first = (hf * HK + 2 * c + k) * R + at
                        r_.pst[l, first : first + STRIP, rows] = e.astype(BF16)
                for k in range(2):
                    h = 2 * c + k
                    left = jnp.concatenate([r_.kvT[l, head_dims(hf, h, D), rows], ones], 0)
                    o = dot_nt(left, r_.pst[l, head_rows(hf, h), rows])
                    r_.odT[i, head_dims(hf, h)] = o[0:HEAD_DIM]
                    r_.ldT[i, head_dims(hf, h)] = o[HEAD_DIM:]
            r_.md[i, :, lanes] = by_head([r_.tp[k] for k in range(HK)])

    def attention_end(l):
        tops = [r_.md[i].T for i in range(NB)]
        top = tops[0]
        for i in range(1, NB):
            top = jnp.maximum(top, tops[i])
        factors = [jnp.exp2((tops[i] - top) * factor_exp) for i in range(NB)]
        inv = 1.0 / sum(factors[i] * r_.ldT[i] for i in range(NB))
        o = jnp.zeros((D, R), F32)
        for i in range(NB):
            r_.rb[l, i] = (factors[i] * inv).T
            o = o + factors[i] * inv * r_.odT[i]
        o = o.T
        r_.oraw[l] = o
        ob = o.astype(BF16)
        r_.ob[l] = ob
        t1 = r_.xf[l] + dot(ob, r_.wo[l])
        r_.z1[l] = t1
        mean1 = col_sum(t1) / R
        return mean1, col_sum((t1 - mean1) * (t1 - mean1))

    def convolution(l):
        xs = r_.xs
        xb = xs[l, me]
        r_.xe[l, 0:R] = xb
        arrive(r_.xe.at[l, R : R + 64], r_.hx_r.at[l])
        xe = r_.xe[l]
        made = dot(xe, r_.wp[l])
        pd_high, pd_low = split(made[:, 2 * D : 3 * D])
        r_.re[0:256] = made[:, 3 * D :].astype(BF16)
        r_.re[256:512] = r_.we[l]
        r_.re[512:768] = pd_high
        r_.re[768:1024] = pd_low
        r_.gate[l] = dot(r_.le[...], r_.re[...])
        r_.bs[l] = dot(r_.le[:, 0:256], made[:, D : 2 * D].astype(BF16)).astype(BF16)
        for at in range(0, E, 64):
            here = slice(at, at + 64)
            gate = sigmoid(r_.gate[l, here])
            r_.gate[l, here] = gate
            high, low = split(jnp.concatenate([gate * r_.bs[l, here].astype(F32), gate], 1))
            r_.gg[here] = high
            r_.gg[E + at : E + at + 64] = low
        num_den = dot(r_.TT[...], r_.gg[...])
        pa, num, den = made[0:R, 0:D], num_den[:, 0:D], num_den[:, D:]
        r_.num[l] = num
        r_.den[l] = den
        msg = pa + num / (den + GATE_EPS)
        r_.z0[l] = msg
        mean0 = col_sum(msg) / R
        return mean0, col_sum((msg - mean0) * (msg - mean0))

    def forward(l):
        def ready(js):
            for j in js:
                moved = (r_.gb[l, j].astype(F32) + r_.moff[j, 0:1]) * r_.move[0:1] + r_.move[1:2]
                r_.xs[l, j] = moved.astype(BF16)

        r_.xs[l, me] = r_.xf[l].astype(BF16)
        r_.hx[l] = dot(r_.HS[...], r_.xs[l, me]).astype(BF16)
        send(r_.hx.at[l, 0:32], r_.xe.at[l, R + 32 : R + 64], r_.hx_s.at[0], r_.hx_r.at[l], nodes=prev)
        send(r_.hx.at[l, 32:64], r_.xe.at[l, R : R + 32], r_.hx_s.at[0], r_.hx_r.at[l], nodes=nxt)
        prepare_queries(l)
        for t in range(2, NZ):
            gather_pass(l, t)
        mean0, sq0 = convolution(l)
        sync_start(3 * l, mean0, sq0)
        gather_near(l)
        ready([partner, 2 * z_from(1) + par, 2 * z_from(1) + 1 - par])

        attention_keys(l, 0)
        attention_heads(l, 0, (0, 1))
        gather_far(l)
        ready([2 * z_from(t) + p for t in range(2, NZ) for p in range(2)])
        for i in range(1, NB):
            attention_keys(l, i)
            attention_heads(l, i, (0, 1))
        mean1, sq1 = attention_end(l)
        sync_start(3 * l + 1, mean1, sq1)
        mean0, sq0 = sync_moments(3 * l)
        inv0 = lax.rsqrt(sq0 / total + NORM_EPS)
        r_.iv[l, 0:1] = inv0
        z0 = (r_.z0[l] - mean0) * inv0
        r_.z0[l] = z0
        n0 = z0 * r_.gain[l, 0:1] + r_.shift[l, 0:1]
        r_.local[...] = r_.xf[l] + n0 * sigmoid(n0)
        mean1, sq1 = sync_moments(3 * l + 1)
        inv1 = lax.rsqrt(sq1 / total + NORM_EPS)
        r_.iv[l, 1:2] = inv1
        z1 = (r_.z1[l] - mean1) * inv1
        r_.z1[l] = z1
        mix = r_.local[...] + z1 * r_.gain[l, 1:2] + r_.shift[l, 1:2]
        mb = mix.astype(BF16)
        r_.mb[l] = mb
        u = dot(mb, r_.wu[l])
        r_.u[l] = u
        g = (u * sigmoid(u)).astype(BF16)
        r_.g[l] = g
        y = mix + dot(g, r_.wd[l])
        r_.z2[l] = y
        mean = col_sum(y) / R
        cent = y - mean
        k = 3 * l + 2
        sync_start(k, mean, col_sum(cent * cent))

        if l < L - 1:
            r_.gb[l + 1, me] = cent.astype(BF16)
            gather_start(l + 1)

        if l == L - 1:
            dy = r_.cot[...].astype(F32)
            sync_start(3 * L, col_sum(dy), col_sum(dy * cent))

        tot_mean, tot_sq = sync_moments(k)
        inv2 = lax.rsqrt(tot_sq / total + NORM_EPS)
        r_.iv[l, 2:3] = inv2
        z2 = (r_.z2[l] - tot_mean) * inv2
        r_.z2[l] = z2
        gain, shift = r_.gain[l, 2:3], r_.shift[l, 2:3]
        r_.xf[l + 1] = z2 * gain + shift

        if l == L - 1:
            sync_wait(3 * L)
            sums, means = r_.st1[3 * L], r_.st1[k][:, 0:2]
            mean = jnp.mean(means, 0)
            dy_sum = jnp.sum(sums[:, 0:2], 0)
            dy_cent = jnp.sum(sums[:, 2:4] + (means - mean) * sums[:, 0:2], 0)
            dy_sum, dy_cent = unpack(jnp.concatenate([dy_sum, dy_cent], 0))
            r_.gshift[l, 2:3] = dy_sum
            r_.ggain[l, 2:3] = dy_cent * inv2

        for j in range(N):
            tile = r_.st1[k, rep * N + j]
            r_.moff[j, 0:1] = jnp.concatenate([tile[0:1], tile[1:2]], 1) - tot_mean
        r_.move[0:1] = inv2 * gain
        r_.move[1:2] = shift

    for l in range(L):
        forward(l)
    act_copy = pltpu.make_async_copy(r_.xf.at[L], r_.out_act, r_.store.at[0])
    act_copy.start()

    def back_feed_forward(l, k):
        s2, g2 = r_.gshift[l, 2:3], r_.ggain[l, 2:3]
        d3 = r_.gain[l, 2:3] * r_.iv[l, 2:3] * (r_.dy[...] - s2 / total - r_.z2[l] * (g2 / total))
        db = d3.astype(BF16)
        dub = (dot_nt(db, r_.wd[l]) * silu_slope(r_.u[l])).astype(BF16)
        dmix = d3 + dot_nt(dub, r_.wu[l])
        r_.dmix[...] = dmix
        n0 = r_.z0[l] * r_.gain[l, 0:1] + r_.shift[l, 0:1]
        gy0 = dmix * silu_slope(n0)
        sync_start(k, col_sum(dmix), col_sum(dmix * r_.z1[l]))
        sync_start(k + 1, col_sum(gy0), col_sum(gy0 * r_.z0[l]))
        r_.gy0[...] = gy0
        at = put(r_.gs_early, l, 512, dot_tn(r_.mb[l], dub))
        put(r_.gs_early, l, at, dot_tn(r_.g[l], db))
        r_.xeT[...] = r_.xe[l].T
        r_.qT[...] = r_.q[l].T

    def back_norms(l, k):
        s1, g1 = sync_sums(k)
        r_.gshift[l, 1:2] = s1
        r_.ggain[l, 1:2] = g1
        dmix = r_.dmix[...]
        d2 = r_.gain[l, 1:2] * r_.iv[l, 1:2] * (dmix - s1 / total - r_.z1[l] * (g1 / total))
        dab = d2.astype(BF16)
        r_.dxo[...] = dmix + d2
        r_.dob[...] = dot_nt(dab, r_.wo[l]).astype(BF16).astype(F32)
        put(r_.gs_early, l, 0, dot_tn(r_.ob[l], dab))
        r_.gkv[...] = jnp.zeros((2 * D, D), F32)
        r_.dqT[...] = jnp.zeros((D, R), F32)

    def back_half(i):
        t1 = (i + 1) % NB
        half = (zh + t1) % NB
        place = (NB - t1) % NB
        return place, half, slice(place * W, (place + 1) * W)

    def back_heads(l, i, hf):
        place, half, rows = back_half(i)
        if True:
            lanes = lane_half(hf)
            dos = r_.dob[:, lanes] * r_.rb[l, place, :, lanes]
            prod = dos * r_.oraw[l, :, lanes]
            for k in range(HK):
                r_.dom[k * R : (k + 1) * R, 0:128] = jnp.where(lane_head == k, dos, 0.0).astype(BF16)
                r_.dom[k * R : (k + 1) * R, 128:256] = jnp.where(lane_head == k, -prod, 0.0).astype(BF16)
            r_.dosT[...] = dos.T.astype(BF16)
            values = slice(D + hf * 128, D + (hf + 1) * 128)
            right = jnp.concatenate([r_.kvT[l, values, rows], jnp.ones((128, W), BF16)], 0)
            for c in range(HK // 2):
                both = slice(2 * c * R, 2 * (c + 1) * R)
                r_.sc[c % 2, 0 : 2 * R] = dot(r_.dom[both], right)
                for k in range(2):
                    for at in range(0, R, STRIP):
                        first = (hf * HK + 2 * c + k) * R + at
                        e = r_.pst[l, first : first + STRIP, rows].astype(F32)
                        ds = e * r_.sc[c % 2, k * R + at : k * R + at + STRIP]
                        r_.dss[(2 * c + k) * R + at : (2 * c + k) * R + at + STRIP] = ds.astype(BF16)
                for k in range(2):
                    h = 2 * c + k
                    mine, dims = slice(h * R, (h + 1) * R), head_dims(hf, h)
                    r_.dqT[dims] += dot_nt(r_.kvT[l, dims, rows], r_.dss[mine])
                    r_.dkv[dims] = (dot(r_.qT[dims], r_.dss[mine]) * scale).astype(BF16)
                    dv = dot(r_.dosT[h * HEAD_DIM : (h + 1) * HEAD_DIM], r_.pst[l, head_rows(hf, h), rows])
                    r_.dkv[head_dims(hf, h, D)] = dv.astype(BF16)

    def back_rows(l, i):
        _, half, _ = back_half(i)
        dx = dot(r_.wqkv[l, :, D:], r_.dkv[...]).T
        r_.dxs[l, pl.ds(2 * half, 2)] = dx.astype(BF16).reshape(2, 2, R, D)

        if i < NB - 1:
            for t in (2 * (i + 1), 2 * (i + 1) + 1):
                zb = z_to(t)
                send_rows(r_.dxs.at[l, zb, 1 - par], r_.rs1.at[l, zb], R,
                          r_.rs_s.at[0], r_.rsp_r.at[l, i, t % 2], nodes=partner)

        else:
            near = z_to(1)
            send_rows(r_.dxs.at[l, z, 1 - par], r_.ro.at[l, 0], R, r_.rs_s.at[0], r_.ro_r.at[l], nodes=partner)
            send_rows(r_.dxs.at[l, near, par], r_.ro.at[l, 1], R, r_.rs_s.at[0], r_.ro_r.at[l], nodes=2 * near + par)
            send_rows(r_.dxs.at[l, near, 1 - par], r_.ro.at[l, 2], R, r_.rs_s.at[0], r_.ro_r.at[l],
                 nodes=2 * near + 1 - par)

        r_.gkv[...] += dot(r_.dkv[...], r_.xs[l, pl.ds(4 * half, 4)].reshape(W, D))

    def pass_on(l, i, t):
        zb = z_to(t)
        arrive(r_.rs1.at[l, zb], r_.rsp_r.at[l, i, t % 2])
        both = r_.dxs[l, zb, par].astype(F32) + r_.rs1[l, zb].astype(F32)
        r_.cs[l, zb] = both.astype(BF16)
        send_rows(r_.cs.at[l, zb], r_.rs2.at[l, z], R, r_.rs_s.at[0], r_.rsc_r.at[l], nodes=2 * zb + par)

    def back_convolution(l, k):
        s0, g0 = unpack(jnp.sum(r_.st1[k + 1], 0))
        r_.gshift[l, 0:1] = s0
        r_.ggain[l, 0:1] = g0
        inv_den = 1.0 / (r_.den[l] + GATE_EPS)
        dm = r_.gain[l, 0:1] * r_.iv[l, 0:1] * (r_.gy0[...] - s0 / total - r_.z0[l] * (g0 / total))
        dnum = dm * inv_den
        dden = -dnum * r_.num[l] * inv_den
        high, low = split(jnp.concatenate([dnum, dden], 1))
        r_.dn[0:R] = high
        r_.dn[256 : 256 + R] = low
        r_.sc[0, 0:E, 0 : 2 * D] = dot(r_.le[:, 512:1024], r_.dn[...])
        for at in range(0, E, 64):
            here = slice(at, at + 64)
            gate, dnum_e = r_.gate[l, here], r_.sc[0, here, 0:D]
            dgp = (dnum_e * r_.bs[l, here].astype(F32) + r_.sc[0, here, D : 2 * D]) * gate * (1.0 - gate)
            r_.gg[here, 0:D] = (dnum_e * gate).astype(BF16)
            r_.gg[here, D:] = dgp.astype(BF16)
        ext = dot(r_.ST[...], r_.gg[0:E]).astype(BF16)
        r_.dproj[0:R, 0:D] = dm.astype(BF16)
        r_.dproj[:, D : 2 * D] = ext[:, 0:D]
        r_.dproj[0:R, 2 * D : 3 * D] = dot(r_.TT[:, 0:E], r_.gg[0:E, D:]).astype(BF16)
        r_.dproj[:, 3 * D :] = ext[:, D:]
        dxe = dot_nt(r_.dproj[...], r_.wp[l])
        r_.hs[l, 0] = dxe[R : R + 32].astype(BF16)
        r_.hs[l, 1] = dxe[R + 32 : R + 64].astype(BF16)
        r_.dxo[...] += dxe[0:R]

    def send_halo(l):
        send(r_.hs.at[l, 0], r_.hr.at[l, 1], r_.hal_s.at[0], r_.hal_r.at[l], nodes=prev)
        send(r_.hs.at[l, 1], r_.hr.at[l, 0], r_.hal_s.at[0], r_.hal_r.at[l], nodes=nxt)

    def conv_weight_grads(l):
        at = put(r_.gs_conv, l, 0, dot(r_.xeT[...], r_.dproj[...]))
        put(r_.gs_conv, l, at, dot(r_.efT[...], r_.gg[0:E, D:]))

    def back_input(l):
        dx = r_.dxo[...]
        dx = dx + r_.dxs[l, z, par].astype(F32)
        arrive(r_.ro.at[l], r_.ro_r.at[l])
        for slot in range(3):
            dx = dx + r_.ro[l, slot].astype(F32)
        if NZ > 2:
            arrive(r_.rs2.at[l, 0 : NZ - 2], r_.rsc_r.at[l])
        for t in range(2, NZ):
            dx = dx + r_.rs2[l, z_from(t)].astype(F32)
        arrive(r_.hr.at[l], r_.hal_r.at[l])
        back = jnp.concatenate(
            [r_.hr[l, 0].astype(F32)[0:24], r_.hr[l, 1].astype(F32)[0:24], jnp.zeros((16, D), F32)], 0
        )
        return dx + dot(r_.A[...], back.astype(BF16))

    r_.dy[...] = r_.cot[...].astype(F32)

    E1, C1, Q1, E0, C0, QK0, V0 = range(len(GROUPS))

    def steps(*pairs):
        return [functools.partial(reduce_step, g, k) for g, k in pairs]

    r_.dy[...] = r_.cot[...].astype(F32)

    def backward(b):
        l = L - 1 - b
        first, last = b == 0, b == L - 1
        k = 3 * L + 1 + 2 * b
        back_feed_forward(l, k)
        when(last, *steps((E1, 4), (C1, 4), (Q1, 2)))
        back_norms(l, k)
        if first:
            when(True, *steps((E1, 0)))
            back_heads(l, 0, 0)
            back_heads(l, 0, 1)
            back_rows(l, 0)
            when(True, *steps((E1, 1)))
            sync_wait(k + 1)
            back_convolution(l, k)
            send_halo(l)
            pass_on(l, 0, 2)
            conv_weight_grads(l)
            when(True, *steps((C1, 0)))
            back_heads(l, 1, 0)
            pass_on(l, 0, 3)
            when(True, *steps((C1, 1)))
            back_heads(l, 1, 1)
            back_rows(l, 1)
        else:
            when(True, *steps((E1, 5), (C1, 5), (Q1, 3), (E0, 0)))
            sync_wait(k + 1)
            back_convolution(l, k)
            send_halo(l)
            when(True, *steps((E0, 1)))
            conv_weight_grads(l)
            when(True, *steps((C0, 0), (E1, 6), (C1, 6), (Q1, 4)))
            back_heads(l, 0, 0)
            when(True, *steps((E0, 2), (C0, 1)))
            back_heads(l, 0, 1)
            back_rows(l, 0)
            when(True, *steps((E0, 3), (C0, 2), (E1, 7), (C1, 7), (Q1, 5)))
            back_heads(l, 1, 0)
            when(True, *steps((E0, 4), (C0, 3), (E1, 8), (C1, 8), (Q1, 6)))
            for t in range(2, NZ):
                pass_on(l, 0, t)
            back_heads(l, 1, 1)
            back_rows(l, 1)
            when(True, *steps((E0, 5), (C0, 4), (Q1, 7)))
        dqb = (r_.dqT[...].T * scale).astype(BF16)
        r_.dxo[...] += dot_nt(dqb, r_.wqkv[l, :, 0:D])
        at = put(r_.gs_qkv, l, 0, dot(r_.xeT[:, 0:R], dqb))
        put(r_.gs_qkv, l, at, r_.gkv[...].T)
        if first:
            when(True, *steps((Q1, 0)))
            dx = back_input(l)
            r_.dy[...] = dx
            below = L - 2
            sync_start(SYNCS - 1, col_sum(dx), col_sum(dx * r_.z2[below]))
            when(True, *steps((E1, 2), (C1, 2), (Q1, 1)))
            s2, g2 = sync_sums(SYNCS - 1)
            r_.gshift[below, 2:3] = s2
            r_.ggain[below, 2:3] = g2
            when(True, *steps((E1, 3), (C1, 3)))

    for b in range(L):
        backward(b)
    for step in steps((QK0, 0), (V0, 0), (E0, 6), (C0, 5), (Q1, 8), (V0, 1), (QK0, 1)):
        step()
    r_.dy[...] = back_input(0)
    in_copy = pltpu.make_async_copy(r_.dy, r_.grad_in, r_.store.at[1])
    in_copy.start()
    for step in steps(
        (C0, 6), (E0, 7), (V0, 2), (QK0, 2),
        (C0, 7), (E0, 8), (V0, 3), (QK0, 3),
        (C0, 8), (V0, 4), (QK0, 4),
    ):
        step()
    for l in range(L):
        for k in range(3):
            r_.ggain_out[k, l : l + 1] = r_.ggain[l, k : k + 1]
            r_.gshift_out[k, l : l + 1] = r_.gshift[l, k : k + 1]
    for g in range(len(GROUPS)):
        reduce_drain(g)
    sent(r_.meta.at[0 : N - 1], r_.meta_s.at[0])
    sent(r_.st1.at[:, 0 : M * N - 1], r_.st_s.at[0])
    sent(r_.gb.at[:, 0 : 3 + 2 * (NZ - 2)], r_.ag_s.at[0])
    sent(r_.gb.at[:, 0 : 2 * (NB - 1) + 3 + NZ - 2], r_.rs_s.at[0])
    sent(r_.hs, r_.hal_s.at[0])
    sent(r_.hx, r_.hx_s.at[0])
    act_copy.wait()
    in_copy.wait()


def finish_kernel(act_h, gin_h, *refs):
    n = len(GROUPS)
    held, (ggain_h, gshift_h), refs = refs[:n], refs[n : n + 2], refs[n + 2 :]
    act_o, gin_o, proj_o, edge_o, qkv_o, out_o, up_o, down_o, ggain_o, gshift_o = refs[:10]
    summed, refs = refs[10 : 10 + n], refs[10 + n :]
    act, gin, proj, edge, qkv, out, up, down, in_sem, out_sem = refs
    loads = [
        pltpu.make_async_copy(src, dst, in_sem.at[i])
        for i, (src, dst) in enumerate(zip(held + (act_h, gin_h), summed + (act, gin), strict=True))
    ]
    for load in loads:
        load.start()
    ggain_o[...] = ggain_h[...]
    gshift_o[...] = gshift_h[...]
    stores = []

    def store(src, dst):
        copy = pltpu.make_async_copy(src, dst, out_sem.at[len(stores)])
        copy.start()
        stores.append(copy)

    def widen(dst, l, g, at, first=0, last=None):
        rows = dst.shape[1]
        for c in range(first, dst.shape[2] // 128 if last is None else last):
            dst[l, :, 128 * c : 128 * (c + 1)] = summed[g][at : at + rows].astype(F32)
            at += rows
        return at

    for g, (name, l, first, rows, _) in enumerate(GROUPS):
        loads[g].wait()
        if name == "early":
            at = widen(out, l, g, 0)
            store(out.at[l], out_o.at[l])
            at = widen(up, l, g, at)
            store(up.at[l], up_o.at[l])
            widen(down, l, g, at)
            store(down.at[l], down_o.at[l])
        elif name == "conv":
            at = widen(proj, l, g, 0)
            store(proj.at[l], proj_o.at[l])
            widen(edge, l, g, at)
            store(edge.at[l], edge_o.at[l])
        else:
            widen(qkv, l, g, 0, first // 256, (first + rows) // 256)
            if first + rows == 1536:
                store(qkv.at[l], qkv_o.at[l])
    for i, (src, dst) in enumerate(((act, act_o), (gin, gin_o))):
        loads[n + i].wait()
        store(src, dst)
    for copy in stores:
        copy.wait()


def fused_device(
    N, M, node_input, edge_feat, graph_ids, edge_src, edge_dst, halo_send, w_proj, w_edge, w_qkv,
    w_out, w_up, w_down, norm_gain, norm_shift, cotangent,
):
    R, D = node_input.shape
    E = edge_feat.shape[0]
    L = w_proj.shape[0]
    names = scratch_list(N, M, L, R, E)
    vmem = pl.BlockSpec(memory_space=pltpu.VMEM)
    hbm = pl.BlockSpec(memory_space=pltpu.HBM)
    shape = jax.ShapeDtypeStruct
    rows = shape((R, D), F32)
    norm = shape((3, L, D), F32)
    groups = [shape((rows_g, 128), BF16) for _, _, _, rows_g, _ in GROUPS]
    outs = pl.pallas_call(
        functools.partial(kernel, N, M, L, tuple(names)),
        out_shape=[rows, rows, *groups, norm, norm],
        in_specs=[hbm] + [vmem] * 4 + [hbm] * 7 + [vmem] * 2 + [hbm],
        out_specs=[hbm] * (2 + len(GROUPS)) + [vmem] * 2,
        scratch_shapes=list(names.values()),
        compiler_params=pltpu.CompilerParams(
            collective_id=0, has_side_effects=True, vmem_limit_bytes=60 << 20
        ),
        name="layers",
    )(node_input, graph_ids, edge_src, edge_dst, halo_send, edge_feat, w_proj, w_edge, w_qkv, w_out, w_up,
      w_down, norm_gain.transpose(1, 0, 2), norm_shift.transpose(1, 0, 2), cotangent)
    weights = [shape(w.shape, F32) for w in (w_proj, w_edge, w_qkv, w_out, w_up, w_down)]
    results = pl.pallas_call(
        finish_kernel,
        out_shape=[rows, rows, *weights, norm, norm],
        in_specs=[hbm] * (2 + len(GROUPS)) + [vmem] * 2,
        out_specs=[hbm] * 8 + [vmem] * 2,
        scratch_shapes=[pltpu.VMEM(s.shape, s.dtype) for s in (*groups, rows, rows, *weights)]
        + [pltpu.SemaphoreType.DMA((len(GROUPS) + 2,)), pltpu.SemaphoreType.DMA((14,))],
        compiler_params=pltpu.CompilerParams(vmem_limit_bytes=60 << 20),
        name="gradients",
    )(*outs)
    ggain, gshift = results[8].transpose(1, 0, 2), results[9].transpose(1, 0, 2)
    return (*results[:8], ggain, gshift)


BLOCK_CAP = 2048


def extended_2(block, sides, width):
    for axis, dim in sides:
        count = lax.axis_size(axis)
        forward = [(i, i + 1) for i in range(count - 1)]
        forward.append((count - 1, 0))
        backward = [(target, source) for source, target in forward]
        low = lax.ppermute(
            lax.slice_in_dim(block, block.shape[dim] - width, None, axis=dim), axis, forward
        )
        high = lax.ppermute(lax.slice_in_dim(block, 0, width, axis=dim), axis, backward)
        block = jnp.concatenate([low, block, high], axis=dim)
    return block


def block_length(total_rows, upper_limit):
    for length in range(min(total_rows, upper_limit), 0, -1):
        if total_rows % length == 0:
            return length
    return 1


def outer_product(left, right):
    return lax.dot_general(
        left, right, (((0,), (0,)), ((), ())), preferred_element_type=jnp.float32
    )


def times_transposed(left, weight):
    return lax.dot_general(
        left, weight, (((1,), (1,)), ((), ())), preferred_element_type=jnp.float32
    )


def forward_product(left, weight):
    return jnp.dot(left, weight, preferred_element_type=jnp.float32)


def silu_slope_plain(inputs):
    logistic = jax.nn.sigmoid(inputs)
    return logistic * (1.0 + inputs * (1.0 - logistic))


def normalize(inputs, gain_row, shift_row, node_total):
    batch_mean = lax.psum(jnp.sum(inputs, 0), ("nodes", "rep")) / node_total
    centred = inputs - batch_mean
    batch_var = lax.psum(jnp.sum(centred * centred, 0), ("nodes", "rep")) / node_total
    inv_std = lax.rsqrt(batch_var + NORM_EPS)
    standard = (inputs - batch_mean) * inv_std
    return (standard * gain_row + shift_row, standard, inv_std)


def normalize_back(grad_out, standard, inv_std, gain_row, node_total):
    shift_grad, gain_grad = lax.psum(
        (jnp.sum(grad_out, 0), jnp.sum(grad_out * standard, 0)), ("nodes", "rep")
    )
    grad_in = (
        gain_row
        * inv_std
        * (grad_out - shift_grad / node_total - standard * gain_grad / node_total)
    )
    return (grad_in, gain_grad, shift_grad)


def exchange_sources(outgoing):
    halo_rows = outgoing.shape[0] // 2
    grown = extended_2(outgoing, (("nodes", 0),), halo_rows)
    return jnp.concatenate([grown[:halo_rows], grown[3 * halo_rows :]], 0)


def return_sources(incoming_grad):
    halo_rows = incoming_grad.shape[0] // 2
    grown = extended_2(incoming_grad.astype(jnp.bfloat16), (("nodes", 0),), halo_rows).astype(
        incoming_grad.dtype
    )
    return jnp.concatenate([grown[:halo_rows], grown[3 * halo_rows :]], 0)


def attend_forward(query_rows, key_rows, value_rows, local_graphs, group_graphs):
    row_count = query_rows.shape[0]
    score_scale = HEAD_DIM ** (-0.5)
    queries = query_rows.reshape(row_count, HEADS, HEAD_DIM)

    def add_piece(carried, kv_piece, first_row):
        key_piece, value_piece = kv_piece
        piece_rows = key_piece.shape[0]
        block_len = block_length(piece_rows, BLOCK_CAP)

        def add_block(block_state, block_index):
            row_max, row_sum, accumulated = block_state
            block_start = block_index * block_len
            key_block = lax.dynamic_slice_in_dim(key_piece, block_start, block_len, 0).reshape(
                block_len, HEADS, HEAD_DIM
            )
            value_block = lax.dynamic_slice_in_dim(value_piece, block_start, block_len, 0).reshape(
                block_len, HEADS, HEAD_DIM
            )
            key_graphs = lax.dynamic_slice_in_dim(
                group_graphs, first_row + block_start, block_len, 0
            )
            same_graph = (local_graphs[:, None] == key_graphs[None, :])[None]
            scores = (
                jnp.einsum("qhd,khd->hqk", queries, key_block, preferred_element_type=jnp.float32)
                * score_scale
            )
            scores = jnp.where(same_graph, scores, NEG)
            new_max = jnp.maximum(row_max, jnp.max(scores, 2))
            weights = jnp.where(same_graph, jnp.exp(scores - new_max[:, :, None]), 0.0)
            factor = jnp.exp(row_max - new_max)
            row_sum = row_sum * factor + jnp.sum(weights, 2)
            contrib = jnp.einsum(
                "hqk,khd->qhd",
                weights.astype(jnp.bfloat16),
                value_block,
                preferred_element_type=jnp.float32,
            )
            accumulated = accumulated * jnp.transpose(factor)[:, :, None] + contrib
            return ((new_max, row_sum, accumulated), None)

        carried, _ = lax.scan(add_block, carried, jnp.arange(piece_rows // block_len))
        return carried

    start_state = (
        jnp.full((HEADS, row_count), NEG, jnp.float32),
        jnp.zeros((HEADS, row_count), jnp.float32),
        jnp.zeros((row_count, HEADS, HEAD_DIM), jnp.float32),
    )
    row_max, row_sum, accumulated = add_piece(
        start_state,
        (
            lax.all_gather(key_rows, "nodes", axis=0, tiled=True),
            lax.all_gather(value_rows, "nodes", axis=0, tiled=True),
        ),
        jnp.int32(0),
    )
    attn_raw = accumulated / jnp.transpose(row_sum)[:, :, None]
    log_sum = row_max + jnp.log(row_sum)
    return (attn_raw, log_sum)


def attend_backward(
    query_rows, key_rows, value_rows, grad_low, attn_raw, log_sum, local_graphs, group_graphs
):
    row_count = query_rows.shape[0]
    model_width = HEADS * HEAD_DIM
    score_scale = HEAD_DIM ** (-0.5)
    queries = query_rows.reshape(row_count, HEADS, HEAD_DIM)
    grad_heads = grad_low.reshape(row_count, HEADS, HEAD_DIM)
    row_delta = jnp.einsum("qhd,qhd->hq", grad_heads.astype(jnp.float32), attn_raw)

    def score_block(key_block, value_block, key_graphs):
        same_graph = (local_graphs[:, None] == key_graphs[None, :])[None]
        scores = (
            jnp.einsum("qhd,khd->hqk", queries, key_block, preferred_element_type=jnp.float32)
            * score_scale
        )
        attn_weights = jnp.exp(jnp.where(same_graph, scores - log_sum[:, :, None], NEG))
        grad_weights = jnp.einsum(
            "qhd,khd->hqk", grad_heads, value_block, preferred_element_type=jnp.float32
        )
        grad_scores = (attn_weights * (grad_weights - row_delta[:, :, None])).astype(jnp.bfloat16)
        return (attn_weights, grad_scores)

    def key_terms(attn_weights, grad_scores, block_len):
        grad_keys = (
            jnp.einsum("hqk,qhd->khd", grad_scores, queries, preferred_element_type=jnp.float32)
            * score_scale
        )
        grad_values = jnp.einsum(
            "hqk,qhd->khd",
            attn_weights.astype(jnp.bfloat16),
            grad_heads,
            preferred_element_type=jnp.float32,
        )
        return jnp.concatenate(
            [
                grad_keys.reshape(block_len, model_width),
                grad_values.reshape(block_len, model_width),
            ],
            1,
        )

    def query_term(grad_scores, key_block):
        return (
            jnp.einsum("hqk,khd->qhd", grad_scores, key_block, preferred_element_type=jnp.float32)
            * score_scale
        )

    group_rows = group_graphs.shape[0]

    def add_piece(carried, kv_piece, first_row):
        key_piece, value_piece = kv_piece
        piece_rows = key_piece.shape[0]
        block_len = block_length(piece_rows, BLOCK_CAP)

        def add_block(block_state, block_index):
            grad_query, buffer = block_state
            block_start = block_index * block_len
            key_block = lax.dynamic_slice_in_dim(key_piece, block_start, block_len, 0).reshape(
                block_len, HEADS, HEAD_DIM
            )
            value_block = lax.dynamic_slice_in_dim(value_piece, block_start, block_len, 0).reshape(
                block_len, HEADS, HEAD_DIM
            )
            place = first_row + block_start
            key_graphs = lax.dynamic_slice_in_dim(group_graphs, place, block_len, 0)
            attn_weights, grad_scores = score_block(key_block, value_block, key_graphs)
            grad_query = grad_query + query_term(grad_scores, key_block)
            block_terms = key_terms(attn_weights, grad_scores, block_len)
            current = lax.dynamic_slice_in_dim(buffer, place, block_len, 0)
            buffer = lax.dynamic_update_slice_in_dim(buffer, current + block_terms, place, 0)
            return ((grad_query, buffer), None)

        carried, _ = lax.scan(add_block, carried, jnp.arange(piece_rows // block_len))
        return carried

    start_state = (
        jnp.zeros((row_count, HEADS, HEAD_DIM), jnp.float32),
        jnp.zeros((group_rows, 2 * model_width), jnp.float32),
    )
    grad_query, buffer = add_piece(
        start_state,
        (
            lax.all_gather(key_rows, "nodes", axis=0, tiled=True),
            lax.all_gather(value_rows, "nodes", axis=0, tiled=True),
        ),
        jnp.int32(0),
    )
    grad_kv = lax.psum_scatter(buffer, "nodes", scatter_dimension=0, tiled=True)
    return (
        grad_query.reshape(row_count, model_width),
        grad_kv[:, :model_width],
        grad_kv[:, model_width:],
    )


def layer_forward(
    hidden, params, edge_feat, edge_src, edge_dst, halo_send, local_graphs, group_graphs, node_total
):
    w_proj, w_edge, w_qkv, w_out, w_up, w_down, norm_gains, norm_shifts = params
    row_count, model_width = hidden.shape
    hidden_low = hidden.astype(jnp.bfloat16)
    projected = forward_product(hidden_low, w_proj)
    self_term = projected[:, :model_width]
    dest_term = projected[:, 2 * model_width : 3 * model_width]
    source_rows = jnp.concatenate(
        [projected[:, model_width : 2 * model_width], projected[:, 3 * model_width :]], 1
    ).astype(jnp.bfloat16)
    incoming = exchange_sources(source_rows[halo_send])
    extended = jnp.concatenate([source_rows, incoming], 0)
    edge_rows = extended[edge_src].astype(jnp.float32)
    source_b = edge_rows[:, :model_width]
    source_e = edge_rows[:, model_width:]
    edge_proj = forward_product(edge_feat, w_edge)
    gating = jax.nn.sigmoid(dest_term[edge_dst] + source_e + edge_proj)
    numerator = jax.ops.segment_sum(gating * source_b, edge_dst, row_count)
    denominator = jax.ops.segment_sum(gating, edge_dst, row_count)
    message = self_term + numerator / (denominator + GATE_EPS)
    normed_one, standard_one, inv_one = normalize(
        message, norm_gains[0], norm_shifts[0], node_total
    )
    local_out = hidden + jax.nn.silu(normed_one)
    qkv_low = forward_product(hidden_low, w_qkv).astype(jnp.bfloat16)
    query_rows = qkv_low[:, :model_width]
    key_rows = qkv_low[:, model_width : 2 * model_width]
    value_rows = qkv_low[:, 2 * model_width :]
    attn_raw, log_sum = attend_forward(query_rows, key_rows, value_rows, local_graphs, group_graphs)
    attn_low = attn_raw.reshape(row_count, model_width).astype(jnp.bfloat16)
    attn_proj = forward_product(attn_low, w_out)
    normed_two, standard_two, inv_two = normalize(
        hidden + attn_proj, norm_gains[1], norm_shifts[1], node_total
    )
    mixed = local_out + normed_two
    mixed_low = mixed.astype(jnp.bfloat16)
    up_proj = forward_product(mixed_low, w_up)
    activated = jax.nn.silu(up_proj).astype(jnp.bfloat16)
    down_proj = forward_product(activated, w_down)
    normed_three, standard_three, inv_three = normalize(
        mixed + down_proj, norm_gains[2], norm_shifts[2], node_total
    )
    saved = (
        hidden_low,
        source_b,
        gating,
        numerator,
        denominator,
        normed_one,
        standard_one,
        inv_one,
        query_rows,
        key_rows,
        value_rows,
        attn_raw,
        log_sum,
        attn_low,
        standard_two,
        inv_two,
        mixed_low,
        up_proj,
        activated,
        standard_three,
        inv_three,
    )
    return (normed_three, saved)


def layer_backward(
    grad_out,
    params,
    saved,
    edge_feat,
    edge_src,
    edge_dst,
    halo_send,
    local_graphs,
    group_graphs,
    node_total,
):
    w_proj, w_edge, w_qkv, w_out, w_up, w_down, norm_gains, norm_shifts = params
    (
        hidden_low,
        source_b,
        gating,
        numerator,
        denominator,
        normed_one,
        standard_one,
        inv_one,
        query_rows,
        key_rows,
        value_rows,
        attn_raw,
        log_sum,
        attn_low,
        standard_two,
        inv_two,
        mixed_low,
        up_proj,
        activated,
        standard_three,
        inv_three,
    ) = saved
    row_count, model_width = grad_out.shape
    grad_three, gain_three, shift_three = normalize_back(
        grad_out, standard_three, inv_three, norm_gains[2], node_total
    )
    down_grad = grad_three.astype(jnp.bfloat16)
    grad_w_down = outer_product(activated, down_grad)
    up_grad = (times_transposed(down_grad, w_down) * silu_slope_plain(up_proj)).astype(jnp.bfloat16)
    grad_w_up = outer_product(mixed_low, up_grad)
    grad_mixed = grad_three + times_transposed(up_grad, w_up)
    grad_two, gain_two, shift_two = normalize_back(
        grad_mixed, standard_two, inv_two, norm_gains[1], node_total
    )
    out_grad = grad_two.astype(jnp.bfloat16)
    grad_w_out = outer_product(attn_low, out_grad)
    attn_grad = times_transposed(out_grad, w_out).astype(jnp.bfloat16)
    grad_query, grad_key, grad_value = attend_backward(
        query_rows, key_rows, value_rows, attn_grad, attn_raw, log_sum, local_graphs, group_graphs
    )
    qkv_grad = jnp.concatenate([grad_query, grad_key, grad_value], 1).astype(jnp.bfloat16)
    grad_w_qkv = outer_product(hidden_low, qkv_grad)
    grad_message, gain_one, shift_one = normalize_back(
        grad_mixed * silu_slope_plain(normed_one), standard_one, inv_one, norm_gains[0], node_total
    )
    shifted = denominator + GATE_EPS
    grad_numer = grad_message / shifted
    grad_denom = -grad_message * numerator / (shifted * shifted)
    numer_edge = grad_numer[edge_dst]
    grad_gate = numer_edge * source_b + grad_denom[edge_dst]
    grad_pre_edge = grad_gate * gating * (1.0 - gating)
    edge_grad = grad_pre_edge.astype(jnp.bfloat16)
    grad_w_edge = outer_product(edge_feat, edge_grad)
    grad_dest = jax.ops.segment_sum(grad_pre_edge, edge_dst, row_count)
    grad_extended = jax.ops.segment_sum(
        jnp.concatenate([numer_edge * gating, grad_pre_edge], 1),
        edge_src,
        row_count + halo_send.shape[0],
    )
    returned = return_sources(grad_extended[row_count:])
    grad_source = grad_extended[:row_count].at[halo_send].add(returned)
    proj_grad = jnp.concatenate(
        [grad_message, grad_source[:, :model_width], grad_dest, grad_source[:, model_width:]], 1
    ).astype(jnp.bfloat16)
    grad_w_proj = outer_product(hidden_low, proj_grad)
    grad_hidden = (
        grad_mixed
        + grad_two
        + times_transposed(proj_grad, w_proj)
        + times_transposed(qkv_grad, w_qkv)
    )
    weight_grads = (grad_w_proj, grad_w_edge, grad_w_qkv, grad_w_out, grad_w_up, grad_w_down)
    return (
        grad_hidden,
        weight_grads,
        jnp.stack([gain_one, gain_two, gain_three]),
        jnp.stack([shift_one, shift_two, shift_three]),
    )


def per_device(
    node_input,
    edge_feat,
    graph_ids,
    edge_src,
    edge_dst,
    halo_send,
    w_proj,
    w_edge,
    w_qkv,
    w_out,
    w_up,
    w_down,
    norm_gain,
    norm_shift,
    cotangent,
):
    group_graphs = lax.all_gather(graph_ids, "nodes", axis=0, tiled=True)
    node_total = node_input.shape[0] * lax.axis_size("nodes") * lax.axis_size("rep")
    layer_count = w_proj.shape[0]
    layer_params = [
        (
            w_proj[layer_index],
            w_edge[layer_index],
            w_qkv[layer_index],
            w_out[layer_index],
            w_up[layer_index],
            w_down[layer_index],
            norm_gain[layer_index],
            norm_shift[layer_index],
        )
        for layer_index in range(layer_count)
    ]
    hidden = node_input.astype(jnp.float32)
    saved_all = []
    for layer_index in range(layer_count):
        hidden, saved = layer_forward(
            hidden,
            layer_params[layer_index],
            edge_feat,
            edge_src,
            edge_dst,
            halo_send,
            graph_ids,
            group_graphs,
            node_total,
        )
        saved_all.append(saved)
    grad_hidden = cotangent.astype(jnp.float32)
    weight_parts = [None] * layer_count
    gain_parts = [None] * layer_count
    shift_parts = [None] * layer_count
    for layer_index in range(layer_count - 1, -1, -1):
        (
            grad_hidden,
            weight_parts[layer_index],
            gain_parts[layer_index],
            shift_parts[layer_index],
        ) = layer_backward(
            grad_hidden,
            layer_params[layer_index],
            saved_all[layer_index],
            edge_feat,
            edge_src,
            edge_dst,
            halo_send,
            graph_ids,
            group_graphs,
            node_total,
        )
    proj_local = jnp.stack([weight_parts[layer_index][0] for layer_index in range(layer_count)])
    edge_local = jnp.stack([weight_parts[layer_index][1] for layer_index in range(layer_count)])
    qkv_local = jnp.stack([weight_parts[layer_index][2] for layer_index in range(layer_count)])
    out_local = jnp.stack([weight_parts[layer_index][3] for layer_index in range(layer_count)])
    up_local = jnp.stack([weight_parts[layer_index][4] for layer_index in range(layer_count)])
    down_local = jnp.stack([weight_parts[layer_index][5] for layer_index in range(layer_count)])
    grad_proj, grad_edge, grad_qkv, grad_out, grad_up, grad_down = lax.psum(
        (proj_local, edge_local, qkv_local, out_local, up_local, down_local), ("nodes", "rep")
    )
    return (
        hidden,
        grad_hidden,
        grad_proj,
        grad_edge,
        grad_qkv,
        grad_out,
        grad_up,
        grad_down,
        jnp.stack(gain_parts),
        jnp.stack(shift_parts),
    )


def solution(mesh):
    in_specs = (
        P(("rep", "nodes"), None),
        P(("rep", "nodes"), None),
        P(("rep", "nodes")),
        P(("rep", "nodes")),
        P(("rep", "nodes")),
        P(("rep", "nodes")),
        P(),
        P(),
        P(),
        P(),
        P(),
        P(),
        P(),
        P(),
        P(("rep", "nodes"), None),
    )
    out_specs = (
        P(("rep", "nodes"), None),
        P(("rep", "nodes"), None),
        P(),
        P(),
        P(),
        P(),
        P(),
        P(),
        P(),
        P(),
    )
    N, M = mesh.shape["nodes"], mesh.shape["rep"]
    fused = N in (4, 8) and M % 2 == 0 and 512 % (16 * N * M) == 0
    return jax.shard_map(
        functools.partial(fused_device, N, M) if fused else per_device,
        mesh=mesh, in_specs=in_specs, out_specs=out_specs, check_vma=False,
    )
```

```python
import functools
import math

import jax
import jax.numpy as jnp
from jax import lax
from jax.experimental import pallas as pl
from jax.experimental.pallas import tpu as pltpu
from jax.sharding import PartitionSpec as P

HEADS = 8
HEAD_DIM = 32
NEG = -1e30
NORM_EPS = 1e-05
GATE_EPS = 1e-06
F32, BF16, I32 = jnp.float32, jnp.bfloat16, jnp.int32
MESH = pl.DeviceIdType.MESH
SYNCS = 12
STRIP = 32
GROUPS = (
    ("early", 1, 0, 2560, ("core", "y", "x", "z")),
    ("conv", 1, 0, 2560, ("core", "y", "x", "z")),
    ("qkv", 1, 0, 1536, ("core", "y", "x", "z")),
    ("early", 0, 0, 2560, ("core", "x", "y", "z")),
    ("conv", 0, 0, 2560, ("core", "x", "y", "z")),
    ("qkv", 0, 0, 1024, ("rep", "nodes")),
    ("qkv", 0, 1024, 512, ("nodes", "rep")),
)


def dot(left, right):
    return lax.dot_general(
        left, right, (((1,), (0,)), ((), ())), preferred_element_type=F32
    )


def dot_nt(left, right):
    return lax.dot_general(
        left, right, (((1,), (1,)), ((), ())), preferred_element_type=F32
    )


def dot_tn(left, right):
    return lax.dot_general(
        left, right, (((0,), (0,)), ((), ())), preferred_element_type=F32
    )


def split(value):
    high = value.astype(BF16)
    return high, (value - high.astype(F32)).astype(BF16)


def sigmoid(value):
    return jax.nn.sigmoid(value)


def silu_slope(value):
    logistic = sigmoid(value)
    return logistic * (1.0 + value * (1.0 - logistic))


def col_sum(value):
    return jnp.sum(value, axis=0, keepdims=True)


def pack(first, second):
    return jnp.concatenate([first[:, :128], first[:, 128:], second[:, :128], second[:, 128:]], 0)


def unpack(tile):
    return [jnp.concatenate([tile[i : i + 1], tile[i + 1 : i + 2]], 1) for i in (0, 2)]


def combine_moments(tiles, count):
    mean = jnp.mean(tiles[:, 0:2], 0)
    off = tiles[:, 0:2] - mean
    return jnp.concatenate([mean, jnp.sum(tiles[:, 2:4] + count * off * off, 0)], 0)


class Refs:
    pass


def axis_sizes(N, M):
    return dict(core=2, y=M // 2, x=2, z=N // 2, rep=M, nodes=N)


def scratch_list(N, M, L, R, E):
    NZ, NB, G = N // 2, N // 4, N * R
    D, FF, W, HH = 256, 512, 4 * R, HEADS // 2 * R
    dma = lambda *shape: pltpu.SemaphoreType.DMA(shape)
    vm = lambda dtype, *shape: pltpu.VMEM(shape, dtype)
    names = dict(
        gb=vm(BF16, L, N, R, D),
        xs=vm(BF16, L, N, R, D),
        meta=vm(I32, N, 8, 256),
        cot=vm(BF16, R, D),
        wp=vm(BF16, L, D, 4 * D),
        we=vm(BF16, L, D, D),
        wqkv=vm(BF16, L, D, 3 * D),
        wo=vm(BF16, L, D, D),
        wu=vm(BF16, L, D, FF),
        wd=vm(BF16, L, FF, D),
        st1=vm(F32, SYNCS, M * N, 4, 128),
        gain=vm(F32, L, 8, D),
        shift=vm(F32, L, 8, D),
        ggain=vm(F32, L, 8, D),
        gshift=vm(F32, L, 8, D),
        iv=vm(F32, L, 8, D),
        moff=vm(F32, N, 8, D),
        move=vm(F32, 8, D),
        le=vm(BF16, E, 1024),
        re=vm(BF16, 1024, D),
        TT=vm(BF16, R, 2 * E),
        ST=vm(BF16, 256, E),
        efT=vm(BF16, D, E),
        HS=vm(BF16, 64, R),
        hx=vm(BF16, L, 64, D),
        A=vm(BF16, R, 64),
        bias=vm(F32, R, G),
        xf=vm(F32, L + 1, R, D),
        xe=vm(BF16, L, 256, D),
        xeT=vm(BF16, D, 256),
        gate=vm(F32, L, E, D),
        bs=vm(BF16, L, E, D),
        num=vm(F32, L, R, D),
        den=vm(F32, L, R, D),
        z0=vm(F32, L, R, D),
        z1=vm(F32, L, R, D),
        z2=vm(F32, L, R, D),
        wkvT=vm(BF16, L, 2 * D, D),
        kvT=vm(BF16, L, 2 * D, G),
        odT=vm(F32, NB, D, R),
        ldT=vm(F32, NB, D, R),
        md=vm(F32, NB, R, D),
        rb=vm(F32, L, NB, R, D),
        pst=vm(BF16, L, HEADS * R, G),
        oraw=vm(F32, L, R, D),
        ob=vm(BF16, L, R, D),
        mb=vm(BF16, L, R, D),
        u=vm(F32, L, R, FF),
        g=vm(BF16, L, R, FF),
        dy=vm(F32, R, D),
        dmix=vm(F32, R, D),
        gy0=vm(F32, R, D),
        local=vm(F32, R, D),
        dxo=vm(F32, R, D),
        dob=vm(F32, R, D),
        dqT=vm(F32, D, R),
        qm=vm(BF16, L, 2, HH, 128),
        q=vm(BF16, L, R, D),
        qT=vm(BF16, D, R),
        dosT=vm(BF16, 128, R),
        dom=vm(BF16, HH, 256),
        sc=vm(F32, 2, max(2 * R, E), W),
        tp=vm(F32, HEADS // 2, R, 128),
        dss=vm(BF16, HH, W),
        dkv=vm(BF16, 2 * D, W),
        gkv=vm(F32, 2 * D, D),
        gg=vm(BF16, 2 * E, 2 * D),
        dn=vm(BF16, 512, 2 * D),
        dproj=vm(BF16, 256, 4 * D),
        dxs=vm(BF16, L, NZ, 2, R, D),
        rs1=vm(BF16, L, NZ, R, D),
        cs=vm(BF16, L, NZ, R, D),
        rs2=vm(BF16, L, NZ, R, D),
        ro=vm(BF16, L, 3, R, D),
        hs=vm(BF16, L, 2, 32, D),
        hr=vm(BF16, L, 2, 32, D),
    )
    names.update(
        gs_early=vm(BF16, L, 2560, 128),
        gs_conv=vm(BF16, L, 2560, 128),
        gs_qkv=vm(BF16, L, 1536, 128),
    )
    sizes = axis_sizes(N, M)
    for g, (_, _, _, rows, stages) in enumerate(GROUPS):
        names[f"go{g}"] = vm(BF16, rows, 128)
        left = rows
        for k, axis in enumerate(stages):
            left //= sizes[axis]
            names[f"ga{g}_{k}"] = vm(BF16, sizes[axis] - 1, left, 128)
            if k < len(stages) - 1:
                names[f"gh{g}_{k}"] = vm(BF16, left, 128)
    names.update(
        ar_s=dma(len(GROUPS)),
        ar_r=dma(sum(2 * len(stages) for *_, stages in GROUPS)),
        ar_l=dma(len(GROUPS)),
        load=dma(9),
        store=dma(2),
        meta_s=dma(1),
        meta_r=dma(1),
        st_s=dma(1),
        st_r=dma(SYNCS),
        ag_s=dma(1),
        agn_r=dma(L),
        agc_r=dma(L, NZ),
        agp_r=dma(L),
        rs_s=dma(1),
        rsp_r=dma(L, NB, 2),
        ro_r=dma(L),
        rsc_r=dma(L),
        hx_s=dma(1),
        hx_r=dma(L),
        hal_s=dma(1),
        hal_r=dma(L),
    )
    return names


IN_NAMES = (
    "x_in", "ids", "edge_src", "edge_dst", "halo", "ef_h", "wp_h", "we_h", "wqkv_h", "wo_h", "wu_h", "wd_h",
    "gain_in", "shift_in", "cot_h",
)
OUT_NAMES = ("out_act", "grad_in", *(f"gout{g}" for g in range(len(GROUPS))), "ggain_out", "gshift_out")


def kernel(N, M, L, names, *args):
    r_ = Refs()
    for name, ref in zip(IN_NAMES + OUT_NAMES + tuple(names), args, strict=True):
        setattr(r_, name, ref)
    R, D = r_.x_in.shape
    E = r_.ef_h.shape[0]
    NZ, NB, G, W = N // 2, N // 4, N * R, 4 * R
    HK = HEADS // 2
    total = float(N * M * R)
    scale = HEAD_DIM ** -0.5
    me = lax.axis_index("nodes")
    rep = lax.axis_index("rep")
    z = me // 2
    par = me % 2
    partner = 2 * z + (1 - par)
    prev = (me + N - 1) % N
    nxt = (me + 1) % N
    zh, zl = z // 2, z % 2
    z_to = lambda t: 2 * ((zh + t // 2) % NB) + (zl + t % 2) % 2
    z_from = lambda t: 2 * ((zh + NB - t // 2) % NB) + (zl + t % 2) % 2

    def remote(src, dst, s_sem, r_sem, **where):
        return pltpu.make_async_remote_copy(
            src_ref=src, dst_ref=dst, send_sem=s_sem, recv_sem=r_sem,
            device_id=where, device_id_type=MESH,
        )

    def send(src, dst, s_sem, r_sem, **where):
        remote(src, dst, s_sem, r_sem, **where).start()

    def send_rows(src, dst, rows, s_sem, r_sem, **where):
        pieces = next(p for p in range(1, rows) if rows % (16 * p) == 0 and rows // p <= 128)
        for at in range(0, rows, rows // pieces):
            cut = pl.ds(at, rows // pieces)
            send(src.at[cut], dst.at[cut], s_sem, r_sem, **where)

    def arrive(dst, r_sem):
        remote(dst, dst, r_sem, r_sem, nodes=partner).wait_recv()

    def sent(src, s_sem):
        remote(src, src, s_sem, s_sem, nodes=partner).wait_send()

    def when(condition, *acts):
        if condition:
            for act in acts:
                act()

    loads = [pltpu.make_async_copy(r_.ef_h, r_.le.at[:, D : 2 * D], r_.load.at[0])] + [
        pltpu.make_async_copy(getattr(r_, f"{name}_h"), getattr(r_, name), r_.load.at[1 + i])
        for i, name in enumerate(("we", "wqkv", "wp", "wo", "wu", "wd", "cot"))
    ]
    own_rows = pltpu.make_async_copy(r_.x_in, r_.gb.at[0, me], r_.load.at[8])
    own_rows.start()
    for load in loads:
        load.start()

    barrier = pltpu.get_barrier_semaphore()
    for dr in range(M):
        for d in range(N):
            if dr + d > 0:
                pl.semaphore_signal(barrier, inc=1, device_id={"rep": (rep + dr) % M, "nodes": (me + d) % N},
                                    device_id_type=MESH)
    pl.semaphore_wait(barrier, M * N - 1)

    def gather_start(l):
        mine = r_.gb.at[l, me]
        for t in range(2, NZ):
            send_rows(mine, mine, R, r_.ag_s.at[0], r_.agc_r.at[l, t], nodes=2 * z_to(t) + par)
        send_rows(mine, mine, R, r_.ag_s.at[0], r_.agn_r.at[l], nodes=partner)
        send_rows(mine, mine, R, r_.ag_s.at[0], r_.agn_r.at[l], nodes=2 * z_to(1) + par)
        send_rows(mine, mine, R, r_.ag_s.at[0], r_.agn_r.at[l], nodes=2 * z_to(1) + 1 - par)

    def gather_pass(l, t):
        piece = r_.gb.at[l, 2 * z_from(t) + par]
        arrive(piece, r_.agc_r.at[l, t])
        send_rows(piece, piece, R, r_.ag_s.at[0], r_.agp_r.at[l], nodes=partner)

    def gather_near(l):
        arrive(r_.gb.at[l, 0:3], r_.agn_r.at[l])

    def gather_far(l):
        arrive(r_.gb.at[l, 0 : NZ - 2], r_.agp_r.at[l])

    def sync_start(k, first, second):
        mine = rep * N + me
        r_.st1[k, mine] = pack(first, second)
        for dr in range(M):
            for d in range(N):
                if dr + d > 0:
                    send(r_.st1.at[k, mine], r_.st1.at[k, mine], r_.st_s.at[0], r_.st_r.at[k],
                         rep=(rep + dr) % M, nodes=(me + d) % N)

    def sync_wait(k):
        arrive(r_.st1.at[k, 0 : M * N - 1], r_.st_r.at[k])

    def sync_moments(k):
        sync_wait(k)
        return unpack(combine_moments(r_.st1[k], float(R)))

    def sync_sums(k):
        sync_wait(k)
        return unpack(jnp.sum(r_.st1[k], 0))

    sizes = axis_sizes(N, M)
    core, row = rep % 2, rep // 2
    places = dict(
        core=(core, lambda t: dict(rep=2 * row + t)),
        y=(row, lambda t: dict(rep=2 * t + core)),
        x=(par, lambda t: dict(nodes=2 * z + t)),
        z=(z, lambda t: dict(nodes=2 * t + par)),
        rep=(rep, lambda t: dict(rep=t)),
        nodes=(me, lambda t: dict(nodes=t)),
    )

    def reduce_step(g, step):
        name, layer, first, rows, stages = GROUPS[g]
        K = len(stages)
        base = sum(2 * len(before) for *_, before in GROUPS[:g])
        gs, out = getattr(r_, f"gs_{name}").at[layer, first : first + rows], getattr(r_, f"go{g}")
        count, offset = [rows], [0]
        for axis in stages:
            count.append(count[-1] // sizes[axis])
            offset.append(offset[-1] + places[axis][0] * count[-1])
        take = lambda start, size: pl.ds(pl.multiple_of(start, 16), size)
        if 1 <= step <= K:
            k = step - 1
            got = getattr(r_, f"ga{g}_{k}")
            arrive(got, r_.ar_r.at[base + k])
            held = gs if k == 0 else getattr(r_, f"gh{g}_{k - 1}")
            index = places[stages[k]][0]
            acc = held[take(index * count[k + 1], count[k + 1])].astype(F32)
            for slot in range(sizes[stages[k]] - 1):
                acc = acc + got[slot].astype(F32)
            if step < K:
                getattr(r_, f"gh{g}_{k}")[...] = acc.astype(BF16)
            else:
                out[take(offset[K], count[K])] = acc.astype(BF16)
        elif step > K:
            k = 2 * K - step
            arrive(out.at[0 : (sizes[stages[k]] - 1) * count[k + 1]], r_.ar_r.at[base + step - 1])
        if step < K:
            held = gs if step == 0 else getattr(r_, f"gh{g}_{step - 1}")
            index, device = places[stages[step]]
            size = sizes[stages[step]]
            for d in range(1, size):
                to = (index + d) % size
                send_rows(held.at[take(to * count[step + 1], count[step + 1])], getattr(r_, f"ga{g}_{step}").at[d - 1],
                     count[step + 1], r_.ar_s.at[g], r_.ar_r.at[base + step], **device(to))
        elif step < 2 * K:
            k = 2 * K - 1 - step
            index, device = places[stages[k]]
            size = sizes[stages[k]]
            here = out.at[take(offset[k + 1], count[k + 1])]
            for d in range(1, size):
                send_rows(here, here, count[k + 1], r_.ar_s.at[g], r_.ar_r.at[base + step],
                          **device((index + d) % size))
        else:
            pltpu.make_async_copy(out, getattr(r_, f"gout{g}"), r_.ar_l.at[g]).start()

    def reduce_drain(g):
        name, _, _, rows, _ = GROUPS[g]
        sent(getattr(r_, f"gs_{name}").at[:, 0 : rows - rows // (M * N)], r_.ar_s.at[g])
        pltpu.make_async_copy(getattr(r_, f"go{g}"), getattr(r_, f"gout{g}"), r_.ar_l.at[g]).wait()

    def put(buf, l, at, value):
        rows = value.shape[0]
        for c in range(value.shape[1] // 128):
            buf[l, at : at + rows] = value[:, 128 * c : 128 * (c + 1)].astype(BF16)
            at += rows
        return at

    lane_head = lax.broadcasted_iota(I32, (R, 128), 1) // HEAD_DIM

    def by_head(parts):
        out = parts[0]
        for k in range(1, HK):
            out = jnp.where(lane_head == k, parts[k], out)
        return out

    r_.meta[me] = jnp.full((8, 256), -1, I32)
    r_.meta[me, 0:1, 0:R] = r_.ids[...].reshape(1, R)
    r_.meta[me, 1:2, 0:48] = r_.halo[...].reshape(1, 48)
    for d in range(1, N):
        send(r_.meta.at[me], r_.meta.at[me], r_.meta_s.at[0], r_.meta_r.at[0], nodes=(me + d) % N)
    own_rows.wait()
    gather_start(0)

    src_row = r_.edge_src[...].reshape(1, E)
    src_row = jnp.where(src_row < R + 24, src_row, src_row + 8)
    dst_row = r_.edge_dst[...].reshape(1, E)
    src_col = jnp.broadcast_to(src_row, (128, E)).T[:, 0:1]
    dst_col = jnp.broadcast_to(dst_row, (128, E)).T[:, 0:1]
    as_mask = lambda cond: cond.astype(F32).astype(BF16)
    r_.le[:, 0:256] = as_mask(src_col == lax.broadcasted_iota(I32, (E, 256), 1))
    target = as_mask(dst_col == lax.broadcasted_iota(I32, (E, 256), 1))
    r_.le[:, 512:768] = target
    r_.le[:, 768:1024] = target
    target = as_mask(dst_row == lax.broadcasted_iota(I32, (R, E), 0))
    r_.TT[:, 0:E] = target
    r_.TT[:, E:] = target
    r_.ST[...] = as_mask(src_row == lax.broadcasted_iota(I32, (256, E), 0))
    r_.dn[R:256] = jnp.zeros((256 - R, 2 * D), BF16)
    r_.dn[256 + R : 512] = jnp.zeros((256 - R, 2 * D), BF16)
    r_.dproj[R:256, 0:D] = jnp.zeros((256 - R, D), BF16)
    r_.dproj[R:256, 2 * D : 3 * D] = jnp.zeros((256 - R, D), BF16)
    halo_col = jnp.broadcast_to(r_.meta[me][1:2, 0:128], (128, 128)).T
    hot = (halo_col[0:48, 0:1] == lax.broadcasted_iota(I32, (48, R), 1)).astype(F32)
    pad = jnp.zeros((8, R), F32)
    r_.HS[...] = jnp.concatenate([hot[0:24], pad, hot[24:48], pad], 0).astype(BF16)
    loads[0].wait()
    r_.efT[...] = r_.le[:, D : 2 * D].T
    for l in range(L):
        for k in range(3):
            r_.gain[l, k : k + 1] = r_.gain_in[k, l : l + 1]
            r_.shift[l, k : k + 1] = r_.shift_in[k, l : l + 1]
    r_.xf[0] = r_.gb[0, me].astype(F32)
    r_.moff[...] = jnp.zeros((N, 8, D), F32)
    r_.move[0:1] = jnp.ones((1, D), F32)
    r_.move[1:2] = jnp.zeros((1, D), F32)
    for load in loads[1:]:
        load.wait()
    for l in range(L):
        r_.wkvT[l] = r_.wqkv[l, :, D:].T

    arrive(r_.meta.at[0 : N - 1], r_.meta_r.at[0])
    id_col = jnp.broadcast_to(r_.meta[me][0:1, 0:R], (128, R)).T[:, 0:1]
    id_row = jnp.concatenate(
        [r_.meta[4 * ((zh + NB - j // 4) % NB) + j % 4][0:1, 0:R] for j in range(N)], 1
    )
    r_.bias[...] = jnp.where(id_col == id_row, 0.0, NEG)

    r_.A[...] = as_mask(r_.meta[me][1:2, 0:64] == lax.broadcasted_iota(I32, (R, 64), 0))

    factor_exp = scale * math.log2(math.e)

    def prepare_queries(l):
        q = dot(r_.xs[l, me], r_.wqkv[l, :, :D]).astype(BF16)
        r_.q[l] = q
        q = q.astype(F32)
        for hf in range(2):
            for k in range(HK):
                part = jnp.where(lane_head == k, q[:, 128 * hf : 128 * (hf + 1)], 0.0)
                r_.qm[l, hf, k * R : (k + 1) * R] = part.astype(BF16)

    def head_dims(hf, k, base=0):
        first = base + hf * 128 + k * HEAD_DIM
        return slice(first, first + HEAD_DIM)

    def head_rows(hf, k, count=1):
        return slice((hf * HK + k) * R, (hf * HK + k + count) * R)

    def lane_half(hf):
        return slice(hf * 128, (hf + 1) * 128)

    def half_of(i):
        return (zh + NB - i) % NB, slice(i * W, (i + 1) * W)

    def attention_keys(l, i):
        half, rows = half_of(i)
        x = r_.xs[l, pl.ds(4 * half, 4)].reshape(W, D)
        r_.kvT[l, :, rows] = dot_nt(r_.wkvT[l], x).astype(BF16)

    def attention_heads(l, i, hfs):
        _, rows = half_of(i)
        for hf in hfs:
            lanes = lane_half(hf)
            ones = jnp.ones((HEAD_DIM, W), BF16)
            for c in range(HK // 2):
                r_.sc[c % 2, 0 : 2 * R] = dot(r_.qm[l, hf, 2 * c * R : 2 * (c + 1) * R], r_.kvT[l, lanes, rows])
                for k in range(2):
                    for at in range(0, R, STRIP):
                        s = r_.sc[c % 2, k * R + at : k * R + at + STRIP] + r_.bias[at : at + STRIP, rows]
                        top = jnp.max(s, 1, keepdims=True)
                        e = jnp.exp2((s - top) * factor_exp)
                        r_.tp[2 * c + k, at : at + STRIP] = jnp.broadcast_to(top, (STRIP, 128))
                        first = (hf * HK + 2 * c + k) * R + at
                        r_.pst[l, first : first + STRIP, rows] = e.astype(BF16)
                for k in range(2):
                    h = 2 * c + k
                    left = jnp.concatenate([r_.kvT[l, head_dims(hf, h, D), rows], ones], 0)
                    o = dot_nt(left, r_.pst[l, head_rows(hf, h), rows])
                    r_.odT[i, head_dims(hf, h)] = o[0:HEAD_DIM]
                    r_.ldT[i, head_dims(hf, h)] = o[HEAD_DIM:]
            r_.md[i, :, lanes] = by_head([r_.tp[k] for k in range(HK)])

    def attention_end(l):
        tops = [r_.md[i].T for i in range(NB)]
        top = tops[0]
        for i in range(1, NB):
            top = jnp.maximum(top, tops[i])
        factors = [jnp.exp2((tops[i] - top) * factor_exp) for i in range(NB)]
        inv = 1.0 / sum(factors[i] * r_.ldT[i] for i in range(NB))
        o = jnp.zeros((D, R), F32)
        for i in range(NB):
            r_.rb[l, i] = (factors[i] * inv).T
            o = o + factors[i] * inv * r_.odT[i]
        o = o.T
        r_.oraw[l] = o
        ob = o.astype(BF16)
        r_.ob[l] = ob
        t1 = r_.xf[l] + dot(ob, r_.wo[l])
        r_.z1[l] = t1
        mean1 = col_sum(t1) / R
        return mean1, col_sum((t1 - mean1) * (t1 - mean1))

    def convolution(l):
        xs = r_.xs
        xb = xs[l, me]
        r_.xe[l, 0:R] = xb
        arrive(r_.xe.at[l, R : R + 64], r_.hx_r.at[l])
        xe = r_.xe[l]
        made = dot(xe, r_.wp[l])
        pd_high, pd_low = split(made[:, 2 * D : 3 * D])
        r_.re[0:256] = made[:, 3 * D :].astype(BF16)
        r_.re[256:512] = r_.we[l]
        r_.re[512:768] = pd_high
        r_.re[768:1024] = pd_low
        r_.gate[l] = dot(r_.le[...], r_.re[...])
        r_.bs[l] = dot(r_.le[:, 0:256], made[:, D : 2 * D].astype(BF16)).astype(BF16)
        for at in range(0, E, 64):
            here = slice(at, at + 64)
            gate = sigmoid(r_.gate[l, here])
            r_.gate[l, here] = gate
            high, low = split(jnp.concatenate([gate * r_.bs[l, here].astype(F32), gate], 1))
            r_.gg[here] = high
            r_.gg[E + at : E + at + 64] = low
        num_den = dot(r_.TT[...], r_.gg[...])
        pa, num, den = made[0:R, 0:D], num_den[:, 0:D], num_den[:, D:]
        r_.num[l] = num
        r_.den[l] = den
        msg = pa + num / (den + GATE_EPS)
        r_.z0[l] = msg
        mean0 = col_sum(msg) / R
        return mean0, col_sum((msg - mean0) * (msg - mean0))

    def forward(l):
        def ready(js):
            for j in js:
                moved = (r_.gb[l, j].astype(F32) + r_.moff[j, 0:1]) * r_.move[0:1] + r_.move[1:2]
                r_.xs[l, j] = moved.astype(BF16)

        r_.xs[l, me] = r_.xf[l].astype(BF16)
        r_.hx[l] = dot(r_.HS[...], r_.xs[l, me]).astype(BF16)
        send(r_.hx.at[l, 0:32], r_.xe.at[l, R + 32 : R + 64], r_.hx_s.at[0], r_.hx_r.at[l], nodes=prev)
        send(r_.hx.at[l, 32:64], r_.xe.at[l, R : R + 32], r_.hx_s.at[0], r_.hx_r.at[l], nodes=nxt)
        prepare_queries(l)
        for t in range(2, NZ):
            gather_pass(l, t)
        mean0, sq0 = convolution(l)
        sync_start(3 * l, mean0, sq0)
        gather_near(l)
        ready([partner, 2 * z_from(1) + par, 2 * z_from(1) + 1 - par])

        attention_keys(l, 0)
        attention_heads(l, 0, (0, 1))
        gather_far(l)
        ready([2 * z_from(t) + p for t in range(2, NZ) for p in range(2)])
        for i in range(1, NB):
            attention_keys(l, i)
            attention_heads(l, i, (0, 1))
        mean1, sq1 = attention_end(l)
        sync_start(3 * l + 1, mean1, sq1)
        mean0, sq0 = sync_moments(3 * l)
        inv0 = lax.rsqrt(sq0 / total + NORM_EPS)
        r_.iv[l, 0:1] = inv0
        z0 = (r_.z0[l] - mean0) * inv0
        r_.z0[l] = z0
        n0 = z0 * r_.gain[l, 0:1] + r_.shift[l, 0:1]
        r_.local[...] = r_.xf[l] + n0 * sigmoid(n0)
        mean1, sq1 = sync_moments(3 * l + 1)
        inv1 = lax.rsqrt(sq1 / total + NORM_EPS)
        r_.iv[l, 1:2] = inv1
        z1 = (r_.z1[l] - mean1) * inv1
        r_.z1[l] = z1
        mix = r_.local[...] + z1 * r_.gain[l, 1:2] + r_.shift[l, 1:2]
        mb = mix.astype(BF16)
        r_.mb[l] = mb
        u = dot(mb, r_.wu[l])
        r_.u[l] = u
        g = (u * sigmoid(u)).astype(BF16)
        r_.g[l] = g
        y = mix + dot(g, r_.wd[l])
        r_.z2[l] = y
        mean = col_sum(y) / R
        cent = y - mean
        k = 3 * l + 2
        sync_start(k, mean, col_sum(cent * cent))

        if l < L - 1:
            r_.gb[l + 1, me] = cent.astype(BF16)
            gather_start(l + 1)

        if l == L - 1:
            dy = r_.cot[...].astype(F32)
            sync_start(3 * L, col_sum(dy), col_sum(dy * cent))

        tot_mean, tot_sq = sync_moments(k)
        inv2 = lax.rsqrt(tot_sq / total + NORM_EPS)
        r_.iv[l, 2:3] = inv2
        z2 = (r_.z2[l] - tot_mean) * inv2
        r_.z2[l] = z2
        gain, shift = r_.gain[l, 2:3], r_.shift[l, 2:3]
        r_.xf[l + 1] = z2 * gain + shift

        if l == L - 1:
            sync_wait(3 * L)
            sums, means = r_.st1[3 * L], r_.st1[k][:, 0:2]
            mean = jnp.mean(means, 0)
            dy_sum = jnp.sum(sums[:, 0:2], 0)
            dy_cent = jnp.sum(sums[:, 2:4] + (means - mean) * sums[:, 0:2], 0)
            dy_sum, dy_cent = unpack(jnp.concatenate([dy_sum, dy_cent], 0))
            r_.gshift[l, 2:3] = dy_sum
            r_.ggain[l, 2:3] = dy_cent * inv2

        for j in range(N):
            tile = r_.st1[k, rep * N + j]
            r_.moff[j, 0:1] = jnp.concatenate([tile[0:1], tile[1:2]], 1) - tot_mean
        r_.move[0:1] = inv2 * gain
        r_.move[1:2] = shift

    for l in range(L):
        forward(l)
    act_copy = pltpu.make_async_copy(r_.xf.at[L], r_.out_act, r_.store.at[0])
    act_copy.start()

    def back_feed_forward(l, k):
        s2, g2 = r_.gshift[l, 2:3], r_.ggain[l, 2:3]
        d3 = r_.gain[l, 2:3] * r_.iv[l, 2:3] * (r_.dy[...] - s2 / total - r_.z2[l] * (g2 / total))
        db = d3.astype(BF16)
        dub = (dot_nt(db, r_.wd[l]) * silu_slope(r_.u[l])).astype(BF16)
        dmix = d3 + dot_nt(dub, r_.wu[l])
        r_.dmix[...] = dmix
        n0 = r_.z0[l] * r_.gain[l, 0:1] + r_.shift[l, 0:1]
        gy0 = dmix * silu_slope(n0)
        sync_start(k, col_sum(dmix), col_sum(dmix * r_.z1[l]))
        sync_start(k + 1, col_sum(gy0), col_sum(gy0 * r_.z0[l]))
        r_.gy0[...] = gy0
        at = put(r_.gs_early, l, 512, dot_tn(r_.mb[l], dub))
        put(r_.gs_early, l, at, dot_tn(r_.g[l], db))
        r_.xeT[...] = r_.xe[l].T
        r_.qT[...] = r_.q[l].T

    def back_norms(l, k):
        s1, g1 = sync_sums(k)
        r_.gshift[l, 1:2] = s1
        r_.ggain[l, 1:2] = g1
        dmix = r_.dmix[...]
        d2 = r_.gain[l, 1:2] * r_.iv[l, 1:2] * (dmix - s1 / total - r_.z1[l] * (g1 / total))
        dab = d2.astype(BF16)
        r_.dxo[...] = dmix + d2
        r_.dob[...] = dot_nt(dab, r_.wo[l]).astype(BF16).astype(F32)
        put(r_.gs_early, l, 0, dot_tn(r_.ob[l], dab))
        r_.gkv[...] = jnp.zeros((2 * D, D), F32)
        r_.dqT[...] = jnp.zeros((D, R), F32)

    def back_half(i):
        t1 = (i + 1) % NB
        half = (zh + t1) % NB
        place = (NB - t1) % NB
        return place, half, slice(place * W, (place + 1) * W)

    def back_heads(l, i, hf):
        place, half, rows = back_half(i)
        if True:
            lanes = lane_half(hf)
            dos = r_.dob[:, lanes] * r_.rb[l, place, :, lanes]
            prod = dos * r_.oraw[l, :, lanes]
            for k in range(HK):
                r_.dom[k * R : (k + 1) * R, 0:128] = jnp.where(lane_head == k, dos, 0.0).astype(BF16)
                r_.dom[k * R : (k + 1) * R, 128:256] = jnp.where(lane_head == k, -prod, 0.0).astype(BF16)
            r_.dosT[...] = dos.T.astype(BF16)
            values = slice(D + hf * 128, D + (hf + 1) * 128)
            right = jnp.concatenate([r_.kvT[l, values, rows], jnp.ones((128, W), BF16)], 0)
            for c in range(HK // 2):
                both = slice(2 * c * R, 2 * (c + 1) * R)
                r_.sc[c % 2, 0 : 2 * R] = dot(r_.dom[both], right)
                for k in range(2):
                    for at in range(0, R, STRIP):
                        first = (hf * HK + 2 * c + k) * R + at
                        e = r_.pst[l, first : first + STRIP, rows].astype(F32)
                        ds = e * r_.sc[c % 2, k * R + at : k * R + at + STRIP]
                        r_.dss[(2 * c + k) * R + at : (2 * c + k) * R + at + STRIP] = ds.astype(BF16)
                for k in range(2):
                    h = 2 * c + k
                    mine, dims = slice(h * R, (h + 1) * R), head_dims(hf, h)
                    r_.dqT[dims] += dot_nt(r_.kvT[l, dims, rows], r_.dss[mine])
                    r_.dkv[dims] = (dot(r_.qT[dims], r_.dss[mine]) * scale).astype(BF16)
                    dv = dot(r_.dosT[h * HEAD_DIM : (h + 1) * HEAD_DIM], r_.pst[l, head_rows(hf, h), rows])
                    r_.dkv[head_dims(hf, h, D)] = dv.astype(BF16)

    def back_rows(l, i):
        _, half, _ = back_half(i)
        dx = dot(r_.wqkv[l, :, D:], r_.dkv[...]).T
        r_.dxs[l, pl.ds(2 * half, 2)] = dx.astype(BF16).reshape(2, 2, R, D)

        if i < NB - 1:
            for t in (2 * (i + 1), 2 * (i + 1) + 1):
                zb = z_to(t)
                send_rows(r_.dxs.at[l, zb, 1 - par], r_.rs1.at[l, zb], R,
                          r_.rs_s.at[0], r_.rsp_r.at[l, i, t % 2], nodes=partner)

        else:
            near = z_to(1)
            send_rows(r_.dxs.at[l, z, 1 - par], r_.ro.at[l, 0], R, r_.rs_s.at[0], r_.ro_r.at[l], nodes=partner)
            send_rows(r_.dxs.at[l, near, par], r_.ro.at[l, 1], R, r_.rs_s.at[0], r_.ro_r.at[l], nodes=2 * near + par)
            send_rows(r_.dxs.at[l, near, 1 - par], r_.ro.at[l, 2], R, r_.rs_s.at[0], r_.ro_r.at[l],
                 nodes=2 * near + 1 - par)

        r_.gkv[...] += dot(r_.dkv[...], r_.xs[l, pl.ds(4 * half, 4)].reshape(W, D))

    def pass_on(l, i, t):
        zb = z_to(t)
        arrive(r_.rs1.at[l, zb], r_.rsp_r.at[l, i, t % 2])
        both = r_.dxs[l, zb, par].astype(F32) + r_.rs1[l, zb].astype(F32)
        r_.cs[l, zb] = both.astype(BF16)
        send_rows(r_.cs.at[l, zb], r_.rs2.at[l, z], R, r_.rs_s.at[0], r_.rsc_r.at[l], nodes=2 * zb + par)

    def back_convolution(l, k):
        s0, g0 = unpack(jnp.sum(r_.st1[k + 1], 0))
        r_.gshift[l, 0:1] = s0
        r_.ggain[l, 0:1] = g0
        inv_den = 1.0 / (r_.den[l] + GATE_EPS)
        dm = r_.gain[l, 0:1] * r_.iv[l, 0:1] * (r_.gy0[...] - s0 / total - r_.z0[l] * (g0 / total))
        dnum = dm * inv_den
        dden = -dnum * r_.num[l] * inv_den
        high, low = split(jnp.concatenate([dnum, dden], 1))
        r_.dn[0:R] = high
        r_.dn[256 : 256 + R] = low
        r_.sc[0, 0:E, 0 : 2 * D] = dot(r_.le[:, 512:1024], r_.dn[...])
        for at in range(0, E, 64):
            here = slice(at, at + 64)
            gate, dnum_e = r_.gate[l, here], r_.sc[0, here, 0:D]
            dgp = (dnum_e * r_.bs[l, here].astype(F32) + r_.sc[0, here, D : 2 * D]) * gate * (1.0 - gate)
            r_.gg[here, 0:D] = (dnum_e * gate).astype(BF16)
            r_.gg[here, D:] = dgp.astype(BF16)
        ext = dot(r_.ST[...], r_.gg[0:E]).astype(BF16)
        r_.dproj[0:R, 0:D] = dm.astype(BF16)
        r_.dproj[:, D : 2 * D] = ext[:, 0:D]
        r_.dproj[0:R, 2 * D : 3 * D] = dot(r_.TT[:, 0:E], r_.gg[0:E, D:]).astype(BF16)
        r_.dproj[:, 3 * D :] = ext[:, D:]
        dxe = dot_nt(r_.dproj[...], r_.wp[l])
        r_.hs[l, 0] = dxe[R : R + 32].astype(BF16)
        r_.hs[l, 1] = dxe[R + 32 : R + 64].astype(BF16)
        r_.dxo[...] += dxe[0:R]

    def send_halo(l):
        send(r_.hs.at[l, 0], r_.hr.at[l, 1], r_.hal_s.at[0], r_.hal_r.at[l], nodes=prev)
        send(r_.hs.at[l, 1], r_.hr.at[l, 0], r_.hal_s.at[0], r_.hal_r.at[l], nodes=nxt)

    def conv_weight_grads(l):
        at = put(r_.gs_conv, l, 0, dot(r_.xeT[...], r_.dproj[...]))
        put(r_.gs_conv, l, at, dot(r_.efT[...], r_.gg[0:E, D:]))

    def back_input(l):
        dx = r_.dxo[...]
        dx = dx + r_.dxs[l, z, par].astype(F32)
        arrive(r_.ro.at[l], r_.ro_r.at[l])
        for slot in range(3):
            dx = dx + r_.ro[l, slot].astype(F32)
        if NZ > 2:
            arrive(r_.rs2.at[l, 0 : NZ - 2], r_.rsc_r.at[l])
        for t in range(2, NZ):
            dx = dx + r_.rs2[l, z_from(t)].astype(F32)
        arrive(r_.hr.at[l], r_.hal_r.at[l])
        back = jnp.concatenate(
            [r_.hr[l, 0].astype(F32)[0:24], r_.hr[l, 1].astype(F32)[0:24], jnp.zeros((16, D), F32)], 0
        )
        return dx + dot(r_.A[...], back.astype(BF16))

    r_.dy[...] = r_.cot[...].astype(F32)

    E1, C1, Q1, E0, C0, QK0, V0 = range(len(GROUPS))

    def steps(*pairs):
        return [functools.partial(reduce_step, g, k) for g, k in pairs]

    r_.dy[...] = r_.cot[...].astype(F32)

    def backward(b):
        l = L - 1 - b
        first, last = b == 0, b == L - 1
        k = 3 * L + 1 + 2 * b
        back_feed_forward(l, k)
        when(last, *steps((E1, 4), (C1, 4), (Q1, 2)))
        back_norms(l, k)
        if first:
            when(True, *steps((E1, 0)))
            back_heads(l, 0, 0)
            back_heads(l, 0, 1)
            back_rows(l, 0)
            when(True, *steps((E1, 1)))
            sync_wait(k + 1)
            back_convolution(l, k)
            send_halo(l)
            pass_on(l, 0, 2)
            conv_weight_grads(l)
            when(True, *steps((C1, 0)))
            back_heads(l, 1, 0)
            pass_on(l, 0, 3)
            when(True, *steps((C1, 1)))
            back_heads(l, 1, 1)
            back_rows(l, 1)
        else:
            when(True, *steps((E1, 5), (C1, 5), (Q1, 3), (E0, 0)))
            sync_wait(k + 1)
            back_convolution(l, k)
            send_halo(l)
            when(True, *steps((E0, 1)))
            conv_weight_grads(l)
            when(True, *steps((C0, 0), (E1, 6), (C1, 6), (Q1, 4)))
            back_heads(l, 0, 0)
            when(True, *steps((E0, 2), (C0, 1)))
            back_heads(l, 0, 1)
            back_rows(l, 0)
            when(True, *steps((E0, 3), (C0, 2), (E1, 7), (C1, 7), (Q1, 5)))
            back_heads(l, 1, 0)
            when(True, *steps((E0, 4), (C0, 3), (E1, 8), (C1, 8), (Q1, 6)))
            for t in range(2, NZ):
                pass_on(l, 0, t)
            back_heads(l, 1, 1)
            back_rows(l, 1)
            when(True, *steps((E0, 5), (C0, 4), (Q1, 7)))
        dqb = (r_.dqT[...].T * scale).astype(BF16)
        r_.dxo[...] += dot_nt(dqb, r_.wqkv[l, :, 0:D])
        at = put(r_.gs_qkv, l, 0, dot(r_.xeT[:, 0:R], dqb))
        put(r_.gs_qkv, l, at, r_.gkv[...].T)
        if first:
            when(True, *steps((Q1, 0)))
            dx = back_input(l)
            r_.dy[...] = dx
            below = L - 2
            sync_start(SYNCS - 1, col_sum(dx), col_sum(dx * r_.z2[below]))
            when(True, *steps((E1, 2), (C1, 2), (Q1, 1)))
            s2, g2 = sync_sums(SYNCS - 1)
            r_.gshift[below, 2:3] = s2
            r_.ggain[below, 2:3] = g2
            when(True, *steps((E1, 3), (C1, 3)))

    for b in range(L):
        backward(b)
    for step in steps((QK0, 0), (V0, 0), (E0, 6), (C0, 5), (Q1, 8), (V0, 1), (QK0, 1)):
        step()
    r_.dy[...] = back_input(0)
    in_copy = pltpu.make_async_copy(r_.dy, r_.grad_in, r_.store.at[1])
    in_copy.start()
    for step in steps(
        (C0, 6), (E0, 7), (V0, 2), (QK0, 2),
        (C0, 7), (E0, 8), (V0, 3), (QK0, 3),
        (C0, 8), (V0, 4), (QK0, 4),
    ):
        step()
    for l in range(L):
        for k in range(3):
            r_.ggain_out[k, l : l + 1] = r_.ggain[l, k : k + 1]
            r_.gshift_out[k, l : l + 1] = r_.gshift[l, k : k + 1]
    for g in range(len(GROUPS)):
        reduce_drain(g)
    sent(r_.meta.at[0 : N - 1], r_.meta_s.at[0])
    sent(r_.st1.at[:, 0 : M * N - 1], r_.st_s.at[0])
    sent(r_.gb.at[:, 0 : 3 + 2 * (NZ - 2)], r_.ag_s.at[0])
    sent(r_.gb.at[:, 0 : 2 * (NB - 1) + 3 + NZ - 2], r_.rs_s.at[0])
    sent(r_.hs, r_.hal_s.at[0])
    sent(r_.hx, r_.hx_s.at[0])
    act_copy.wait()
    in_copy.wait()


def finish_kernel(act_h, gin_h, *refs):
    n = len(GROUPS)
    held, (ggain_h, gshift_h), refs = refs[:n], refs[n : n + 2], refs[n + 2 :]
    act_o, gin_o, proj_o, edge_o, qkv_o, out_o, up_o, down_o, ggain_o, gshift_o = refs[:10]
    summed, refs = refs[10 : 10 + n], refs[10 + n :]
    act, gin, proj, edge, qkv, out, up, down, in_sem, out_sem = refs
    loads = [
        pltpu.make_async_copy(src, dst, in_sem.at[i])
        for i, (src, dst) in enumerate(zip(held + (act_h, gin_h), summed + (act, gin), strict=True))
    ]
    for load in loads:
        load.start()
    ggain_o[...] = ggain_h[...]
    gshift_o[...] = gshift_h[...]
    stores = []

    def store(src, dst):
        copy = pltpu.make_async_copy(src, dst, out_sem.at[len(stores)])
        copy.start()
        stores.append(copy)

    def widen(dst, l, g, at, first=0, last=None):
        rows = dst.shape[1]
        for c in range(first, dst.shape[2] // 128 if last is None else last):
            dst[l, :, 128 * c : 128 * (c + 1)] = summed[g][at : at + rows].astype(F32)
            at += rows
        return at

    for g, (name, l, first, rows, _) in enumerate(GROUPS):
        loads[g].wait()
        if name == "early":
            at = widen(out, l, g, 0)
            store(out.at[l], out_o.at[l])
            at = widen(up, l, g, at)
            store(up.at[l], up_o.at[l])
            widen(down, l, g, at)
            store(down.at[l], down_o.at[l])
        elif name == "conv":
            at = widen(proj, l, g, 0)
            store(proj.at[l], proj_o.at[l])
            widen(edge, l, g, at)
            store(edge.at[l], edge_o.at[l])
        else:
            widen(qkv, l, g, 0, first // 256, (first + rows) // 256)
            if first + rows == 1536:
                store(qkv.at[l], qkv_o.at[l])
    for i, (src, dst) in enumerate(((act, act_o), (gin, gin_o))):
        loads[n + i].wait()
        store(src, dst)
    for copy in stores:
        copy.wait()


def fused_device(
    N, M, node_input, edge_feat, graph_ids, edge_src, edge_dst, halo_send, w_proj, w_edge, w_qkv,
    w_out, w_up, w_down, norm_gain, norm_shift, cotangent,
):
    R, D = node_input.shape
    E = edge_feat.shape[0]
    L = w_proj.shape[0]
    names = scratch_list(N, M, L, R, E)
    vmem = pl.BlockSpec(memory_space=pltpu.VMEM)
    hbm = pl.BlockSpec(memory_space=pltpu.HBM)
    shape = jax.ShapeDtypeStruct
    rows = shape((R, D), F32)
    norm = shape((3, L, D), F32)
    groups = [shape((rows_g, 128), BF16) for _, _, _, rows_g, _ in GROUPS]
    outs = pl.pallas_call(
        functools.partial(kernel, N, M, L, tuple(names)),
        out_shape=[rows, rows, *groups, norm, norm],
        in_specs=[hbm] + [vmem] * 4 + [hbm] * 7 + [vmem] * 2 + [hbm],
        out_specs=[hbm] * (2 + len(GROUPS)) + [vmem] * 2,
        scratch_shapes=list(names.values()),
        compiler_params=pltpu.CompilerParams(
            collective_id=0, has_side_effects=True, vmem_limit_bytes=60 << 20
        ),
        name="layers",
    )(node_input, graph_ids, edge_src, edge_dst, halo_send, edge_feat, w_proj, w_edge, w_qkv, w_out, w_up,
      w_down, norm_gain.transpose(1, 0, 2), norm_shift.transpose(1, 0, 2), cotangent)
    weights = [shape(w.shape, F32) for w in (w_proj, w_edge, w_qkv, w_out, w_up, w_down)]
    results = pl.pallas_call(
        finish_kernel,
        out_shape=[rows, rows, *weights, norm, norm],
        in_specs=[hbm] * (2 + len(GROUPS)) + [vmem] * 2,
        out_specs=[hbm] * 8 + [vmem] * 2,
        scratch_shapes=[pltpu.VMEM(s.shape, s.dtype) for s in (*groups, rows, rows, *weights)]
        + [pltpu.SemaphoreType.DMA((len(GROUPS) + 2,)), pltpu.SemaphoreType.DMA((14,))],
        compiler_params=pltpu.CompilerParams(vmem_limit_bytes=60 << 20),
        name="gradients",
    )(*outs)
    ggain, gshift = results[8].transpose(1, 0, 2), results[9].transpose(1, 0, 2)
    return (*results[:8], ggain, gshift)


BLOCK_CAP = 2048


def extended_2(block, sides, width):
    for axis, dim in sides:
        count = lax.axis_size(axis)
        forward = [(i, i + 1) for i in range(count - 1)]
        forward.append((count - 1, 0))
        backward = [(target, source) for source, target in forward]
        low = lax.ppermute(
            lax.slice_in_dim(block, block.shape[dim] - width, None, axis=dim), axis, forward
        )
        high = lax.ppermute(lax.slice_in_dim(block, 0, width, axis=dim), axis, backward)
        block = jnp.concatenate([low, block, high], axis=dim)
    return block


def block_length(total_rows, upper_limit):
    for length in range(min(total_rows, upper_limit), 0, -1):
        if total_rows % length == 0:
            return length
    return 1


def outer_product(left, right):
    return lax.dot_general(
        left, right, (((0,), (0,)), ((), ())), preferred_element_type=jnp.float32
    )


def times_transposed(left, weight):
    return lax.dot_general(
        left, weight, (((1,), (1,)), ((), ())), preferred_element_type=jnp.float32
    )


def forward_product(left, weight):
    return jnp.dot(left, weight, preferred_element_type=jnp.float32)


def silu_slope_plain(inputs):
    logistic = jax.nn.sigmoid(inputs)
    return logistic * (1.0 + inputs * (1.0 - logistic))


def normalize(inputs, gain_row, shift_row, node_total):
    batch_mean = lax.psum(jnp.sum(inputs, 0), ("nodes", "rep")) / node_total
    centred = inputs - batch_mean
    batch_var = lax.psum(jnp.sum(centred * centred, 0), ("nodes", "rep")) / node_total
    inv_std = lax.rsqrt(batch_var + NORM_EPS)
    standard = (inputs - batch_mean) * inv_std
    return (standard * gain_row + shift_row, standard, inv_std)


def normalize_back(grad_out, standard, inv_std, gain_row, node_total):
    shift_grad, gain_grad = lax.psum(
        (jnp.sum(grad_out, 0), jnp.sum(grad_out * standard, 0)), ("nodes", "rep")
    )
    grad_in = (
        gain_row
        * inv_std
        * (grad_out - shift_grad / node_total - standard * gain_grad / node_total)
    )
    return (grad_in, gain_grad, shift_grad)


def exchange_sources(outgoing):
    halo_rows = outgoing.shape[0] // 2
    grown = extended_2(outgoing, (("nodes", 0),), halo_rows)
    return jnp.concatenate([grown[:halo_rows], grown[3 * halo_rows :]], 0)


def return_sources(incoming_grad):
    halo_rows = incoming_grad.shape[0] // 2
    grown = extended_2(incoming_grad.astype(jnp.bfloat16), (("nodes", 0),), halo_rows).astype(
        incoming_grad.dtype
    )
    return jnp.concatenate([grown[:halo_rows], grown[3 * halo_rows :]], 0)


def attend_forward(query_rows, key_rows, value_rows, local_graphs, group_graphs):
    row_count = query_rows.shape[0]
    score_scale = HEAD_DIM ** (-0.5)
    queries = query_rows.reshape(row_count, HEADS, HEAD_DIM)

    def add_piece(carried, kv_piece, first_row):
        key_piece, value_piece = kv_piece
        piece_rows = key_piece.shape[0]
        block_len = block_length(piece_rows, BLOCK_CAP)

        def add_block(block_state, block_index):
            row_max, row_sum, accumulated = block_state
            block_start = block_index * block_len
            key_block = lax.dynamic_slice_in_dim(key_piece, block_start, block_len, 0).reshape(
                block_len, HEADS, HEAD_DIM
            )
            value_block = lax.dynamic_slice_in_dim(value_piece, block_start, block_len, 0).reshape(
                block_len, HEADS, HEAD_DIM
            )
            key_graphs = lax.dynamic_slice_in_dim(
                group_graphs, first_row + block_start, block_len, 0
            )
            same_graph = (local_graphs[:, None] == key_graphs[None, :])[None]
            scores = (
                jnp.einsum("qhd,khd->hqk", queries, key_block, preferred_element_type=jnp.float32)
                * score_scale
            )
            scores = jnp.where(same_graph, scores, NEG)
            new_max = jnp.maximum(row_max, jnp.max(scores, 2))
            weights = jnp.where(same_graph, jnp.exp(scores - new_max[:, :, None]), 0.0)
            factor = jnp.exp(row_max - new_max)
            row_sum = row_sum * factor + jnp.sum(weights, 2)
            contrib = jnp.einsum(
                "hqk,khd->qhd",
                weights.astype(jnp.bfloat16),
                value_block,
                preferred_element_type=jnp.float32,
            )
            accumulated = accumulated * jnp.transpose(factor)[:, :, None] + contrib
            return ((new_max, row_sum, accumulated), None)

        carried, _ = lax.scan(add_block, carried, jnp.arange(piece_rows // block_len))
        return carried

    start_state = (
        jnp.full((HEADS, row_count), NEG, jnp.float32),
        jnp.zeros((HEADS, row_count), jnp.float32),
        jnp.zeros((row_count, HEADS, HEAD_DIM), jnp.float32),
    )
    row_max, row_sum, accumulated = add_piece(
        start_state,
        (
            lax.all_gather(key_rows, "nodes", axis=0, tiled=True),
            lax.all_gather(value_rows, "nodes", axis=0, tiled=True),
        ),
        jnp.int32(0),
    )
    attn_raw = accumulated / jnp.transpose(row_sum)[:, :, None]
    log_sum = row_max + jnp.log(row_sum)
    return (attn_raw, log_sum)


def attend_backward(
    query_rows, key_rows, value_rows, grad_low, attn_raw, log_sum, local_graphs, group_graphs
):
    row_count = query_rows.shape[0]
    model_width = HEADS * HEAD_DIM
    score_scale = HEAD_DIM ** (-0.5)
    queries = query_rows.reshape(row_count, HEADS, HEAD_DIM)
    grad_heads = grad_low.reshape(row_count, HEADS, HEAD_DIM)
    row_delta = jnp.einsum("qhd,qhd->hq", grad_heads.astype(jnp.float32), attn_raw)

    def score_block(key_block, value_block, key_graphs):
        same_graph = (local_graphs[:, None] == key_graphs[None, :])[None]
        scores = (
            jnp.einsum("qhd,khd->hqk", queries, key_block, preferred_element_type=jnp.float32)
            * score_scale
        )
        attn_weights = jnp.exp(jnp.where(same_graph, scores - log_sum[:, :, None], NEG))
        grad_weights = jnp.einsum(
            "qhd,khd->hqk", grad_heads, value_block, preferred_element_type=jnp.float32
        )
        grad_scores = (attn_weights * (grad_weights - row_delta[:, :, None])).astype(jnp.bfloat16)
        return (attn_weights, grad_scores)

    def key_terms(attn_weights, grad_scores, block_len):
        grad_keys = (
            jnp.einsum("hqk,qhd->khd", grad_scores, queries, preferred_element_type=jnp.float32)
            * score_scale
        )
        grad_values = jnp.einsum(
            "hqk,qhd->khd",
            attn_weights.astype(jnp.bfloat16),
            grad_heads,
            preferred_element_type=jnp.float32,
        )
        return jnp.concatenate(
            [
                grad_keys.reshape(block_len, model_width),
                grad_values.reshape(block_len, model_width),
            ],
            1,
        )

    def query_term(grad_scores, key_block):
        return (
            jnp.einsum("hqk,khd->qhd", grad_scores, key_block, preferred_element_type=jnp.float32)
            * score_scale
        )

    group_rows = group_graphs.shape[0]

    def add_piece(carried, kv_piece, first_row):
        key_piece, value_piece = kv_piece
        piece_rows = key_piece.shape[0]
        block_len = block_length(piece_rows, BLOCK_CAP)

        def add_block(block_state, block_index):
            grad_query, buffer = block_state
            block_start = block_index * block_len
            key_block = lax.dynamic_slice_in_dim(key_piece, block_start, block_len, 0).reshape(
                block_len, HEADS, HEAD_DIM
            )
            value_block = lax.dynamic_slice_in_dim(value_piece, block_start, block_len, 0).reshape(
                block_len, HEADS, HEAD_DIM
            )
            place = first_row + block_start
            key_graphs = lax.dynamic_slice_in_dim(group_graphs, place, block_len, 0)
            attn_weights, grad_scores = score_block(key_block, value_block, key_graphs)
            grad_query = grad_query + query_term(grad_scores, key_block)
            block_terms = key_terms(attn_weights, grad_scores, block_len)
            current = lax.dynamic_slice_in_dim(buffer, place, block_len, 0)
            buffer = lax.dynamic_update_slice_in_dim(buffer, current + block_terms, place, 0)
            return ((grad_query, buffer), None)

        carried, _ = lax.scan(add_block, carried, jnp.arange(piece_rows // block_len))
        return carried

    start_state = (
        jnp.zeros((row_count, HEADS, HEAD_DIM), jnp.float32),
        jnp.zeros((group_rows, 2 * model_width), jnp.float32),
    )
    grad_query, buffer = add_piece(
        start_state,
        (
            lax.all_gather(key_rows, "nodes", axis=0, tiled=True),
            lax.all_gather(value_rows, "nodes", axis=0, tiled=True),
        ),
        jnp.int32(0),
    )
    grad_kv = lax.psum_scatter(buffer, "nodes", scatter_dimension=0, tiled=True)
    return (
        grad_query.reshape(row_count, model_width),
        grad_kv[:, :model_width],
        grad_kv[:, model_width:],
    )


def layer_forward(
    hidden, params, edge_feat, edge_src, edge_dst, halo_send, local_graphs, group_graphs, node_total
):
    w_proj, w_edge, w_qkv, w_out, w_up, w_down, norm_gains, norm_shifts = params
    row_count, model_width = hidden.shape
    hidden_low = hidden.astype(jnp.bfloat16)
    projected = forward_product(hidden_low, w_proj)
    self_term = projected[:, :model_width]
    dest_term = projected[:, 2 * model_width : 3 * model_width]
    source_rows = jnp.concatenate(
        [projected[:, model_width : 2 * model_width], projected[:, 3 * model_width :]], 1
    ).astype(jnp.bfloat16)
    incoming = exchange_sources(source_rows[halo_send])
    extended = jnp.concatenate([source_rows, incoming], 0)
    edge_rows = extended[edge_src].astype(jnp.float32)
    source_b = edge_rows[:, :model_width]
    source_e = edge_rows[:, model_width:]
    edge_proj = forward_product(edge_feat, w_edge)
    gating = jax.nn.sigmoid(dest_term[edge_dst] + source_e + edge_proj)
    numerator = jax.ops.segment_sum(gating * source_b, edge_dst, row_count)
    denominator = jax.ops.segment_sum(gating, edge_dst, row_count)
    message = self_term + numerator / (denominator + GATE_EPS)
    normed_one, standard_one, inv_one = normalize(
        message, norm_gains[0], norm_shifts[0], node_total
    )
    local_out = hidden + jax.nn.silu(normed_one)
    qkv_low = forward_product(hidden_low, w_qkv).astype(jnp.bfloat16)
    query_rows = qkv_low[:, :model_width]
    key_rows = qkv_low[:, model_width : 2 * model_width]
    value_rows = qkv_low[:, 2 * model_width :]
    attn_raw, log_sum = attend_forward(query_rows, key_rows, value_rows, local_graphs, group_graphs)
    attn_low = attn_raw.reshape(row_count, model_width).astype(jnp.bfloat16)
    attn_proj = forward_product(attn_low, w_out)
    normed_two, standard_two, inv_two = normalize(
        hidden + attn_proj, norm_gains[1], norm_shifts[1], node_total
    )
    mixed = local_out + normed_two
    mixed_low = mixed.astype(jnp.bfloat16)
    up_proj = forward_product(mixed_low, w_up)
    activated = jax.nn.silu(up_proj).astype(jnp.bfloat16)
    down_proj = forward_product(activated, w_down)
    normed_three, standard_three, inv_three = normalize(
        mixed + down_proj, norm_gains[2], norm_shifts[2], node_total
    )
    saved = (
        hidden_low,
        source_b,
        gating,
        numerator,
        denominator,
        normed_one,
        standard_one,
        inv_one,
        query_rows,
        key_rows,
        value_rows,
        attn_raw,
        log_sum,
        attn_low,
        standard_two,
        inv_two,
        mixed_low,
        up_proj,
        activated,
        standard_three,
        inv_three,
    )
    return (normed_three, saved)


def layer_backward(
    grad_out,
    params,
    saved,
    edge_feat,
    edge_src,
    edge_dst,
    halo_send,
    local_graphs,
    group_graphs,
    node_total,
):
    w_proj, w_edge, w_qkv, w_out, w_up, w_down, norm_gains, norm_shifts = params
    (
        hidden_low,
        source_b,
        gating,
        numerator,
        denominator,
        normed_one,
        standard_one,
        inv_one,
        query_rows,
        key_rows,
        value_rows,
        attn_raw,
        log_sum,
        attn_low,
        standard_two,
        inv_two,
        mixed_low,
        up_proj,
        activated,
        standard_three,
        inv_three,
    ) = saved
    row_count, model_width = grad_out.shape
    grad_three, gain_three, shift_three = normalize_back(
        grad_out, standard_three, inv_three, norm_gains[2], node_total
    )
    down_grad = grad_three.astype(jnp.bfloat16)
    grad_w_down = outer_product(activated, down_grad)
    up_grad = (times_transposed(down_grad, w_down) * silu_slope_plain(up_proj)).astype(jnp.bfloat16)
    grad_w_up = outer_product(mixed_low, up_grad)
    grad_mixed = grad_three + times_transposed(up_grad, w_up)
    grad_two, gain_two, shift_two = normalize_back(
        grad_mixed, standard_two, inv_two, norm_gains[1], node_total
    )
    out_grad = grad_two.astype(jnp.bfloat16)
    grad_w_out = outer_product(attn_low, out_grad)
    attn_grad = times_transposed(out_grad, w_out).astype(jnp.bfloat16)
    grad_query, grad_key, grad_value = attend_backward(
        query_rows, key_rows, value_rows, attn_grad, attn_raw, log_sum, local_graphs, group_graphs
    )
    qkv_grad = jnp.concatenate([grad_query, grad_key, grad_value], 1).astype(jnp.bfloat16)
    grad_w_qkv = outer_product(hidden_low, qkv_grad)
    grad_message, gain_one, shift_one = normalize_back(
        grad_mixed * silu_slope_plain(normed_one), standard_one, inv_one, norm_gains[0], node_total
    )
    shifted = denominator + GATE_EPS
    grad_numer = grad_message / shifted
    grad_denom = -grad_message * numerator / (shifted * shifted)
    numer_edge = grad_numer[edge_dst]
    grad_gate = numer_edge * source_b + grad_denom[edge_dst]
    grad_pre_edge = grad_gate * gating * (1.0 - gating)
    edge_grad = grad_pre_edge.astype(jnp.bfloat16)
    grad_w_edge = outer_product(edge_feat, edge_grad)
    grad_dest = jax.ops.segment_sum(grad_pre_edge, edge_dst, row_count)
    grad_extended = jax.ops.segment_sum(
        jnp.concatenate([numer_edge * gating, grad_pre_edge], 1),
        edge_src,
        row_count + halo_send.shape[0],
    )
    returned = return_sources(grad_extended[row_count:])
    grad_source = grad_extended[:row_count].at[halo_send].add(returned)
    proj_grad = jnp.concatenate(
        [grad_message, grad_source[:, :model_width], grad_dest, grad_source[:, model_width:]], 1
    ).astype(jnp.bfloat16)
    grad_w_proj = outer_product(hidden_low, proj_grad)
    grad_hidden = (
        grad_mixed
        + grad_two
        + times_transposed(proj_grad, w_proj)
        + times_transposed(qkv_grad, w_qkv)
    )
    weight_grads = (grad_w_proj, grad_w_edge, grad_w_qkv, grad_w_out, grad_w_up, grad_w_down)
    return (
        grad_hidden,
        weight_grads,
        jnp.stack([gain_one, gain_two, gain_three]),
        jnp.stack([shift_one, shift_two, shift_three]),
    )


def per_device(
    node_input,
    edge_feat,
    graph_ids,
    edge_src,
    edge_dst,
    halo_send,
    w_proj,
    w_edge,
    w_qkv,
    w_out,
    w_up,
    w_down,
    norm_gain,
    norm_shift,
    cotangent,
):
    group_graphs = lax.all_gather(graph_ids, "nodes", axis=0, tiled=True)
    node_total = node_input.shape[0] * lax.axis_size("nodes") * lax.axis_size("rep")
    layer_count = w_proj.shape[0]
    layer_params = [
        (
            w_proj[layer_index],
            w_edge[layer_index],
            w_qkv[layer_index],
            w_out[layer_index],
            w_up[layer_index],
            w_down[layer_index],
            norm_gain[layer_index],
            norm_shift[layer_index],
        )
        for layer_index in range(layer_count)
    ]
    hidden = node_input.astype(jnp.float32)
    saved_all = []
    for layer_index in range(layer_count):
        hidden, saved = layer_forward(
            hidden,
            layer_params[layer_index],
            edge_feat,
            edge_src,
            edge_dst,
            halo_send,
            graph_ids,
            group_graphs,
            node_total,
        )
        saved_all.append(saved)
    grad_hidden = cotangent.astype(jnp.float32)
    weight_parts = [None] * layer_count
    gain_parts = [None] * layer_count
    shift_parts = [None] * layer_count
    for layer_index in range(layer_count - 1, -1, -1):
        (
            grad_hidden,
            weight_parts[layer_index],
            gain_parts[layer_index],
            shift_parts[layer_index],
        ) = layer_backward(
            grad_hidden,
            layer_params[layer_index],
            saved_all[layer_index],
            edge_feat,
            edge_src,
            edge_dst,
            halo_send,
            graph_ids,
            group_graphs,
            node_total,
        )
    proj_local = jnp.stack([weight_parts[layer_index][0] for layer_index in range(layer_count)])
    edge_local = jnp.stack([weight_parts[layer_index][1] for layer_index in range(layer_count)])
    qkv_local = jnp.stack([weight_parts[layer_index][2] for layer_index in range(layer_count)])
    out_local = jnp.stack([weight_parts[layer_index][3] for layer_index in range(layer_count)])
    up_local = jnp.stack([weight_parts[layer_index][4] for layer_index in range(layer_count)])
    down_local = jnp.stack([weight_parts[layer_index][5] for layer_index in range(layer_count)])
    grad_proj, grad_edge, grad_qkv, grad_out, grad_up, grad_down = lax.psum(
        (proj_local, edge_local, qkv_local, out_local, up_local, down_local), ("nodes", "rep")
    )
    return (
        hidden,
        grad_hidden,
        grad_proj,
        grad_edge,
        grad_qkv,
        grad_out,
        grad_up,
        grad_down,
        jnp.stack(gain_parts),
        jnp.stack(shift_parts),
    )


def solution(mesh):
    in_specs = (
        P(("rep", "nodes"), None),
        P(("rep", "nodes"), None),
        P(("rep", "nodes")),
        P(("rep", "nodes")),
        P(("rep", "nodes")),
        P(("rep", "nodes")),
        P(),
        P(),
        P(),
        P(),
        P(),
        P(),
        P(),
        P(),
        P(("rep", "nodes"), None),
    )
    out_specs = (
        P(("rep", "nodes"), None),
        P(("rep", "nodes"), None),
        P(),
        P(),
        P(),
        P(),
        P(),
        P(),
        P(),
        P(),
    )
    N, M = mesh.shape["nodes"], mesh.shape["rep"]
    fused = N in (4, 8) and M % 2 == 0 and 512 % (16 * N * M) == 0
    return jax.shard_map(
        functools.partial(fused_device, N, M) if fused else per_device,
        mesh=mesh, in_specs=in_specs, out_specs=out_specs, check_vma=False,
    )
```

```python
import functools
import math

import jax
import jax.numpy as jnp
from jax import lax
from jax.experimental import pallas as pl
from jax.experimental.pallas import tpu as pltpu
from jax.sharding import PartitionSpec as P

HEADS = 8
HEAD_DIM = 32
NEG = -1e30
NORM_EPS = 1e-05
GATE_EPS = 1e-06
F32, BF16, I32 = jnp.float32, jnp.bfloat16, jnp.int32
MESH = pl.DeviceIdType.MESH
SYNCS = 12
STRIP = 32
GROUPS = (
    ("early", 1, 0, 2560, ("core", "y", "x", "z")),
    ("conv", 1, 0, 2560, ("core", "y", "x", "z")),
    ("qkv", 1, 0, 1536, ("core", "y", "x", "z")),
    ("early", 0, 0, 2560, ("core", "x", "y", "z")),
    ("conv", 0, 0, 2560, ("core", "x", "y", "z")),
    ("qkv", 0, 0, 1024, ("rep", "nodes")),
    ("qkv", 0, 1024, 512, ("nodes", "rep")),
)


def dot(left, right):
    return lax.dot_general(
        left, right, (((1,), (0,)), ((), ())), preferred_element_type=F32
    )


def dot_nt(left, right):
    return lax.dot_general(
        left, right, (((1,), (1,)), ((), ())), preferred_element_type=F32
    )


def dot_tn(left, right):
    return lax.dot_general(
        left, right, (((0,), (0,)), ((), ())), preferred_element_type=F32
    )


def split(value):
    high = value.astype(BF16)
    return high, (value - high.astype(F32)).astype(BF16)


def sigmoid(value):
    return jax.nn.sigmoid(value)


def silu_slope(value):
    logistic = sigmoid(value)
    return logistic * (1.0 + value * (1.0 - logistic))


def col_sum(value):
    return jnp.sum(value, axis=0, keepdims=True)


def pack(first, second):
    return jnp.concatenate([first[:, :128], first[:, 128:], second[:, :128], second[:, 128:]], 0)


def unpack(tile):
    return [jnp.concatenate([tile[i : i + 1], tile[i + 1 : i + 2]], 1) for i in (0, 2)]


def combine_moments(tiles, count):
    mean = jnp.mean(tiles[:, 0:2], 0)
    off = tiles[:, 0:2] - mean
    return jnp.concatenate([mean, jnp.sum(tiles[:, 2:4] + count * off * off, 0)], 0)


class Refs:
    pass


def axis_sizes(N, M):
    return dict(core=2, y=M // 2, x=2, z=N // 2, rep=M, nodes=N)


def scratch_list(N, M, L, R, E):
    NZ, NB, G = N // 2, N // 4, N * R
    D, FF, W, HH = 256, 512, 4 * R, HEADS // 2 * R
    dma = lambda *shape: pltpu.SemaphoreType.DMA(shape)
    vm = lambda dtype, *shape: pltpu.VMEM(shape, dtype)
    names = dict(
        gb=vm(BF16, L, N, R, D),
        xs=vm(BF16, L, N, R, D),
        meta=vm(I32, N, 8, 256),
        cot=vm(BF16, R, D),
        wp=vm(BF16, L, D, 4 * D),
        we=vm(BF16, L, D, D),
        wqkv=vm(BF16, L, D, 3 * D),
        wo=vm(BF16, L, D, D),
        wu=vm(BF16, L, D, FF),
        wd=vm(BF16, L, FF, D),
        st1=vm(F32, SYNCS, M * N, 4, 128),
        gain=vm(F32, L, 8, D),
        shift=vm(F32, L, 8, D),
        ggain=vm(F32, L, 8, D),
        gshift=vm(F32, L, 8, D),
        iv=vm(F32, L, 8, D),
        moff=vm(F32, N, 8, D),
        move=vm(F32, 8, D),
        le=vm(BF16, E, 1024),
        re=vm(BF16, 1024, D),
        TT=vm(BF16, R, 2 * E),
        ST=vm(BF16, 256, E),
        efT=vm(BF16, D, E),
        HS=vm(BF16, 64, R),
        hx=vm(BF16, L, 64, D),
        A=vm(BF16, R, 64),
        bias=vm(F32, R, G),
        xf=vm(F32, L + 1, R, D),
        xe=vm(BF16, L, 256, D),
        xeT=vm(BF16, D, 256),
        gate=vm(F32, L, E, D),
        bs=vm(BF16, L, E, D),
        num=vm(F32, L, R, D),
        den=vm(F32, L, R, D),
        z0=vm(F32, L, R, D),
        z1=vm(F32, L, R, D),
        z2=vm(F32, L, R, D),
        wkvT=vm(BF16, L, 2 * D, D),
        kvT=vm(BF16, L, 2 * D, G),
        odT=vm(F32, NB, D, R),
        ldT=vm(F32, NB, D, R),
        md=vm(F32, NB, R, D),
        rb=vm(F32, L, NB, R, D),
        pst=vm(BF16, L, HEADS * R, G),
        oraw=vm(F32, L, R, D),
        ob=vm(BF16, L, R, D),
        mb=vm(BF16, L, R, D),
        u=vm(F32, L, R, FF),
        g=vm(BF16, L, R, FF),
        dy=vm(F32, R, D),
        dmix=vm(F32, R, D),
        gy0=vm(F32, R, D),
        local=vm(F32, R, D),
        dxo=vm(F32, R, D),
        dob=vm(F32, R, D),
        dqT=vm(F32, D, R),
        qm=vm(BF16, L, 2, HH, 128),
        q=vm(BF16, L, R, D),
        qT=vm(BF16, D, R),
        dosT=vm(BF16, 128, R),
        dom=vm(BF16, HH, 256),
        sc=vm(F32, 2, max(2 * R, E), W),
        tp=vm(F32, HEADS // 2, R, 128),
        dss=vm(BF16, HH, W),
        dkv=vm(BF16, 2 * D, W),
        gkv=vm(F32, 2 * D, D),
        gg=vm(BF16, 2 * E, 2 * D),
        dn=vm(BF16, 512, 2 * D),
        dproj=vm(BF16, 256, 4 * D),
        dxs=vm(BF16, L, NZ, 2, R, D),
        rs1=vm(BF16, L, NZ, R, D),
        cs=vm(BF16, L, NZ, R, D),
        rs2=vm(BF16, L, NZ, R, D),
        ro=vm(BF16, L, 3, R, D),
        hs=vm(BF16, L, 2, 32, D),
        hr=vm(BF16, L, 2, 32, D),
    )
    names.update(
        gs_early=vm(BF16, L, 2560, 128),
        gs_conv=vm(BF16, L, 2560, 128),
        gs_qkv=vm(BF16, L, 1536, 128),
    )
    sizes = axis_sizes(N, M)
    for g, (_, _, _, rows, stages) in enumerate(GROUPS):
        names[f"go{g}"] = vm(BF16, rows, 128)
        left = rows
        for k, axis in enumerate(stages):
            left //= sizes[axis]
            names[f"ga{g}_{k}"] = vm(BF16, sizes[axis] - 1, left, 128)
            if k < len(stages) - 1:
                names[f"gh{g}_{k}"] = vm(BF16, left, 128)
    names.update(
        ar_s=dma(len(GROUPS)),
        ar_r=dma(sum(2 * len(stages) for *_, stages in GROUPS)),
        ar_l=dma(len(GROUPS)),
        load=dma(9),
        store=dma(2),
        meta_s=dma(1),
        meta_r=dma(1),
        st_s=dma(1),
        st_r=dma(SYNCS),
        ag_s=dma(1),
        agn_r=dma(L),
        agc_r=dma(L, NZ),
        agp_r=dma(L),
        rs_s=dma(1),
        rsp_r=dma(L, NB, 2),
        ro_r=dma(L),
        rsc_r=dma(L),
        hx_s=dma(1),
        hx_r=dma(L),
        hal_s=dma(1),
        hal_r=dma(L),
    )
    return names


IN_NAMES = (
    "x_in", "ids", "edge_src", "edge_dst", "halo", "ef_h", "wp_h", "we_h", "wqkv_h", "wo_h", "wu_h", "wd_h",
    "gain_in", "shift_in", "cot_h",
)
OUT_NAMES = ("out_act", "grad_in", *(f"gout{g}" for g in range(len(GROUPS))), "ggain_out", "gshift_out")


def kernel(N, M, L, names, *args):
    r_ = Refs()
    for name, ref in zip(IN_NAMES + OUT_NAMES + tuple(names), args, strict=True):
        setattr(r_, name, ref)
    R, D = r_.x_in.shape
    E = r_.ef_h.shape[0]
    NZ, NB, G, W = N // 2, N // 4, N * R, 4 * R
    HK = HEADS // 2
    total = float(N * M * R)
    scale = HEAD_DIM ** -0.5
    me = lax.axis_index("nodes")
    rep = lax.axis_index("rep")
    z = me // 2
    par = me % 2
    partner = 2 * z + (1 - par)
    prev = (me + N - 1) % N
    nxt = (me + 1) % N
    zh, zl = z // 2, z % 2
    z_to = lambda t: 2 * ((zh + t // 2) % NB) + (zl + t % 2) % 2
    z_from = lambda t: 2 * ((zh + NB - t // 2) % NB) + (zl + t % 2) % 2

    def remote(src, dst, s_sem, r_sem, **where):
        return pltpu.make_async_remote_copy(
            src_ref=src, dst_ref=dst, send_sem=s_sem, recv_sem=r_sem,
            device_id=where, device_id_type=MESH,
        )

    def send(src, dst, s_sem, r_sem, **where):
        remote(src, dst, s_sem, r_sem, **where).start()

    def send_rows(src, dst, rows, s_sem, r_sem, **where):
        pieces = next(p for p in range(1, rows) if rows % (16 * p) == 0 and rows // p <= 128)
        for at in range(0, rows, rows // pieces):
            cut = pl.ds(at, rows // pieces)
            send(src.at[cut], dst.at[cut], s_sem, r_sem, **where)

    def arrive(dst, r_sem):
        remote(dst, dst, r_sem, r_sem, nodes=partner).wait_recv()

    def sent(src, s_sem):
        remote(src, src, s_sem, s_sem, nodes=partner).wait_send()

    def when(condition, *acts):
        if condition:
            for act in acts:
                act()

    loads = [pltpu.make_async_copy(r_.ef_h, r_.le.at[:, D : 2 * D], r_.load.at[0])] + [
        pltpu.make_async_copy(getattr(r_, f"{name}_h"), getattr(r_, name), r_.load.at[1 + i])
        for i, name in enumerate(("we", "wqkv", "wp", "wo", "wu", "wd", "cot"))
    ]
    own_rows = pltpu.make_async_copy(r_.x_in, r_.gb.at[0, me], r_.load.at[8])
    own_rows.start()
    for load in loads:
        load.start()

    barrier = pltpu.get_barrier_semaphore()
    for dr in range(M):
        for d in range(N):
            if dr + d > 0:
                pl.semaphore_signal(barrier, inc=1, device_id={"rep": (rep + dr) % M, "nodes": (me + d) % N},
                                    device_id_type=MESH)
    pl.semaphore_wait(barrier, M * N - 1)

    def gather_start(l):
        mine = r_.gb.at[l, me]
        for t in range(2, NZ):
            send_rows(mine, mine, R, r_.ag_s.at[0], r_.agc_r.at[l, t], nodes=2 * z_to(t) + par)
        send_rows(mine, mine, R, r_.ag_s.at[0], r_.agn_r.at[l], nodes=partner)
        send_rows(mine, mine, R, r_.ag_s.at[0], r_.agn_r.at[l], nodes=2 * z_to(1) + par)
        send_rows(mine, mine, R, r_.ag_s.at[0], r_.agn_r.at[l], nodes=2 * z_to(1) + 1 - par)

    def gather_pass(l, t):
        piece = r_.gb.at[l, 2 * z_from(t) + par]
        arrive(piece, r_.agc_r.at[l, t])
        send_rows(piece, piece, R, r_.ag_s.at[0], r_.agp_r.at[l], nodes=partner)

    def gather_near(l):
        arrive(r_.gb.at[l, 0:3], r_.agn_r.at[l])

    def gather_far(l):
        arrive(r_.gb.at[l, 0 : NZ - 2], r_.agp_r.at[l])

    def sync_start(k, first, second):
        mine = rep * N + me
        r_.st1[k, mine] = pack(first, second)
        for dr in range(M):
            for d in range(N):
                if dr + d > 0:
                    send(r_.st1.at[k, mine], r_.st1.at[k, mine], r_.st_s.at[0], r_.st_r.at[k],
                         rep=(rep + dr) % M, nodes=(me + d) % N)

    def sync_wait(k):
        arrive(r_.st1.at[k, 0 : M * N - 1], r_.st_r.at[k])

    def sync_moments(k):
        sync_wait(k)
        return unpack(combine_moments(r_.st1[k], float(R)))

    def sync_sums(k):
        sync_wait(k)
        return unpack(jnp.sum(r_.st1[k], 0))

    sizes = axis_sizes(N, M)
    core, row = rep % 2, rep // 2
    places = dict(
        core=(core, lambda t: dict(rep=2 * row + t)),
        y=(row, lambda t: dict(rep=2 * t + core)),
        x=(par, lambda t: dict(nodes=2 * z + t)),
        z=(z, lambda t: dict(nodes=2 * t + par)),
        rep=(rep, lambda t: dict(rep=t)),
        nodes=(me, lambda t: dict(nodes=t)),
    )

    def reduce_step(g, step):
        name, layer, first, rows, stages = GROUPS[g]
        K = len(stages)
        base = sum(2 * len(before) for *_, before in GROUPS[:g])
        gs, out = getattr(r_, f"gs_{name}").at[layer, first : first + rows], getattr(r_, f"go{g}")
        count, offset = [rows], [0]
        for axis in stages:
            count.append(count[-1] // sizes[axis])
            offset.append(offset[-1] + places[axis][0] * count[-1])
        take = lambda start, size: pl.ds(pl.multiple_of(start, 16), size)
        if 1 <= step <= K:
            k = step - 1
            got = getattr(r_, f"ga{g}_{k}")
            arrive(got, r_.ar_r.at[base + k])
            held = gs if k == 0 else getattr(r_, f"gh{g}_{k - 1}")
            index = places[stages[k]][0]
            acc = held[take(index * count[k + 1], count[k + 1])].astype(F32)
            for slot in range(sizes[stages[k]] - 1):
                acc = acc + got[slot].astype(F32)
            if step < K:
                getattr(r_, f"gh{g}_{k}")[...] = acc.astype(BF16)
            else:
                out[take(offset[K], count[K])] = acc.astype(BF16)
        elif step > K:
            k = 2 * K - step
            arrive(out.at[0 : (sizes[stages[k]] - 1) * count[k + 1]], r_.ar_r.at[base + step - 1])
        if step < K:
            held = gs if step == 0 else getattr(r_, f"gh{g}_{step - 1}")
            index, device = places[stages[step]]
            size = sizes[stages[step]]
            for d in range(1, size):
                to = (index + d) % size
                send_rows(held.at[take(to * count[step + 1], count[step + 1])], getattr(r_, f"ga{g}_{step}").at[d - 1],
                     count[step + 1], r_.ar_s.at[g], r_.ar_r.at[base + step], **device(to))
        elif step < 2 * K:
            k = 2 * K - 1 - step
            index, device = places[stages[k]]
            size = sizes[stages[k]]
            here = out.at[take(offset[k + 1], count[k + 1])]
            for d in range(1, size):
                send_rows(here, here, count[k + 1], r_.ar_s.at[g], r_.ar_r.at[base + step],
                          **device((index + d) % size))
        else:
            pltpu.make_async_copy(out, getattr(r_, f"gout{g}"), r_.ar_l.at[g]).start()

    def reduce_drain(g):
        name, _, _, rows, _ = GROUPS[g]
        sent(getattr(r_, f"gs_{name}").at[:, 0 : rows - rows // (M * N)], r_.ar_s.at[g])
        pltpu.make_async_copy(getattr(r_, f"go{g}"), getattr(r_, f"gout{g}"), r_.ar_l.at[g]).wait()

    def put(buf, l, at, value):
        rows = value.shape[0]
        for c in range(value.shape[1] // 128):
            buf[l, at : at + rows] = value[:, 128 * c : 128 * (c + 1)].astype(BF16)
            at += rows
        return at

    lane_head = lax.broadcasted_iota(I32, (R, 128), 1) // HEAD_DIM

    def by_head(parts):
        out = parts[0]
        for k in range(1, HK):
            out = jnp.where(lane_head == k, parts[k], out)
        return out

    r_.meta[me] = jnp.full((8, 256), -1, I32)
    r_.meta[me, 0:1, 0:R] = r_.ids[...].reshape(1, R)
    r_.meta[me, 1:2, 0:48] = r_.halo[...].reshape(1, 48)
    for d in range(1, N):
        send(r_.meta.at[me], r_.meta.at[me], r_.meta_s.at[0], r_.meta_r.at[0], nodes=(me + d) % N)
    own_rows.wait()
    gather_start(0)

    src_row = r_.edge_src[...].reshape(1, E)
    src_row = jnp.where(src_row < R + 24, src_row, src_row + 8)
    dst_row = r_.edge_dst[...].reshape(1, E)
    src_col = jnp.broadcast_to(src_row, (128, E)).T[:, 0:1]
    dst_col = jnp.broadcast_to(dst_row, (128, E)).T[:, 0:1]
    as_mask = lambda cond: cond.astype(F32).astype(BF16)
    r_.le[:, 0:256] = as_mask(src_col == lax.broadcasted_iota(I32, (E, 256), 1))
    target = as_mask(dst_col == lax.broadcasted_iota(I32, (E, 256), 1))
    r_.le[:, 512:768] = target
    r_.le[:, 768:1024] = target
    target = as_mask(dst_row == lax.broadcasted_iota(I32, (R, E), 0))
    r_.TT[:, 0:E] = target
    r_.TT[:, E:] = target
    r_.ST[...] = as_mask(src_row == lax.broadcasted_iota(I32, (256, E), 0))
    r_.dn[R:256] = jnp.zeros((256 - R, 2 * D), BF16)
    r_.dn[256 + R : 512] = jnp.zeros((256 - R, 2 * D), BF16)
    r_.dproj[R:256, 0:D] = jnp.zeros((256 - R, D), BF16)
    r_.dproj[R:256, 2 * D : 3 * D] = jnp.zeros((256 - R, D), BF16)
    halo_col = jnp.broadcast_to(r_.meta[me][1:2, 0:128], (128, 128)).T
    hot = (halo_col[0:48, 0:1] == lax.broadcasted_iota(I32, (48, R), 1)).astype(F32)
    pad = jnp.zeros((8, R), F32)
    r_.HS[...] = jnp.concatenate([hot[0:24], pad, hot[24:48], pad], 0).astype(BF16)
    loads[0].wait()
    r_.efT[...] = r_.le[:, D : 2 * D].T
    for l in range(L):
        for k in range(3):
            r_.gain[l, k : k + 1] = r_.gain_in[k, l : l + 1]
            r_.shift[l, k : k + 1] = r_.shift_in[k, l : l + 1]
    r_.xf[0] = r_.gb[0, me].astype(F32)
    r_.moff[...] = jnp.zeros((N, 8, D), F32)
    r_.move[0:1] = jnp.ones((1, D), F32)
    r_.move[1:2] = jnp.zeros((1, D), F32)
    for load in loads[1:]:
        load.wait()
    for l in range(L):
        r_.wkvT[l] = r_.wqkv[l, :, D:].T

    arrive(r_.meta.at[0 : N - 1], r_.meta_r.at[0])
    id_col = jnp.broadcast_to(r_.meta[me][0:1, 0:R], (128, R)).T[:, 0:1]
    id_row = jnp.concatenate(
        [r_.meta[4 * ((zh + NB - j // 4) % NB) + j % 4][0:1, 0:R] for j in range(N)], 1
    )
    r_.bias[...] = jnp.where(id_col == id_row, 0.0, NEG)

    r_.A[...] = as_mask(r_.meta[me][1:2, 0:64] == lax.broadcasted_iota(I32, (R, 64), 0))

    factor_exp = scale * math.log2(math.e)

    def prepare_queries(l):
        q = dot(r_.xs[l, me], r_.wqkv[l, :, :D]).astype(BF16)
        r_.q[l] = q
        q = q.astype(F32)
        for hf in range(2):
            for k in range(HK):
                part = jnp.where(lane_head == k, q[:, 128 * hf : 128 * (hf + 1)], 0.0)
                r_.qm[l, hf, k * R : (k + 1) * R] = part.astype(BF16)

    def head_dims(hf, k, base=0):
        first = base + hf * 128 + k * HEAD_DIM
        return slice(first, first + HEAD_DIM)

    def head_rows(hf, k, count=1):
        return slice((hf * HK + k) * R, (hf * HK + k + count) * R)

    def lane_half(hf):
        return slice(hf * 128, (hf + 1) * 128)

    def half_of(i):
        return (zh + NB - i) % NB, slice(i * W, (i + 1) * W)

    def attention_keys(l, i):
        half, rows = half_of(i)
        x = r_.xs[l, pl.ds(4 * half, 4)].reshape(W, D)
        r_.kvT[l, :, rows] = dot_nt(r_.wkvT[l], x).astype(BF16)

    def attention_heads(l, i, hfs):
        _, rows = half_of(i)
        for hf in hfs:
            lanes = lane_half(hf)
            ones = jnp.ones((HEAD_DIM, W), BF16)
            for c in range(HK // 2):
                r_.sc[c % 2, 0 : 2 * R] = dot(r_.qm[l, hf, 2 * c * R : 2 * (c + 1) * R], r_.kvT[l, lanes, rows])
                for k in range(2):
                    for at in range(0, R, STRIP):
                        s = r_.sc[c % 2, k * R + at : k * R + at + STRIP] + r_.bias[at : at + STRIP, rows]
                        top = jnp.max(s, 1, keepdims=True)
                        e = jnp.exp2((s - top) * factor_exp)
                        r_.tp[2 * c + k, at : at + STRIP] = jnp.broadcast_to(top, (STRIP, 128))
                        first = (hf * HK + 2 * c + k) * R + at
                        r_.pst[l, first : first + STRIP, rows] = e.astype(BF16)
                for k in range(2):
                    h = 2 * c + k
                    left = jnp.concatenate([r_.kvT[l, head_dims(hf, h, D), rows], ones], 0)
                    o = dot_nt(left, r_.pst[l, head_rows(hf, h), rows])
                    r_.odT[i, head_dims(hf, h)] = o[0:HEAD_DIM]
                    r_.ldT[i, head_dims(hf, h)] = o[HEAD_DIM:]
            r_.md[i, :, lanes] = by_head([r_.tp[k] for k in range(HK)])

    def attention_end(l):
        tops = [r_.md[i].T for i in range(NB)]
        top = tops[0]
        for i in range(1, NB):
            top = jnp.maximum(top, tops[i])
        factors = [jnp.exp2((tops[i] - top) * factor_exp) for i in range(NB)]
        inv = 1.0 / sum(factors[i] * r_.ldT[i] for i in range(NB))
        o = jnp.zeros((D, R), F32)
        for i in range(NB):
            r_.rb[l, i] = (factors[i] * inv).T
            o = o + factors[i] * inv * r_.odT[i]
        o = o.T
        r_.oraw[l] = o
        ob = o.astype(BF16)
        r_.ob[l] = ob
        t1 = r_.xf[l] + dot(ob, r_.wo[l])
        r_.z1[l] = t1
        mean1 = col_sum(t1) / R
        return mean1, col_sum((t1 - mean1) * (t1 - mean1))

    def convolution(l):
        xs = r_.xs
        xb = xs[l, me]
        r_.xe[l, 0:R] = xb
        arrive(r_.xe.at[l, R : R + 64], r_.hx_r.at[l])
        xe = r_.xe[l]
        made = dot(xe, r_.wp[l])
        pd_high, pd_low = split(made[:, 2 * D : 3 * D])
        r_.re[0:256] = made[:, 3 * D :].astype(BF16)
        r_.re[256:512] = r_.we[l]
        r_.re[512:768] = pd_high
        r_.re[768:1024] = pd_low
        r_.gate[l] = dot(r_.le[...], r_.re[...])
        r_.bs[l] = dot(r_.le[:, 0:256], made[:, D : 2 * D].astype(BF16)).astype(BF16)
        for at in range(0, E, 64):
            here = slice(at, at + 64)
            gate = sigmoid(r_.gate[l, here])
            r_.gate[l, here] = gate
            high, low = split(jnp.concatenate([gate * r_.bs[l, here].astype(F32), gate], 1))
            r_.gg[here] = high
            r_.gg[E + at : E + at + 64] = low
        num_den = dot(r_.TT[...], r_.gg[...])
        pa, num, den = made[0:R, 0:D], num_den[:, 0:D], num_den[:, D:]
        r_.num[l] = num
        r_.den[l] = den
        msg = pa + num / (den + GATE_EPS)
        r_.z0[l] = msg
        mean0 = col_sum(msg) / R
        return mean0, col_sum((msg - mean0) * (msg - mean0))

    def forward(l):
        def ready(js):
            for j in js:
                moved = (r_.gb[l, j].astype(F32) + r_.moff[j, 0:1]) * r_.move[0:1] + r_.move[1:2]
                r_.xs[l, j] = moved.astype(BF16)

        r_.xs[l, me] = r_.xf[l].astype(BF16)
        r_.hx[l] = dot(r_.HS[...], r_.xs[l, me]).astype(BF16)
        send(r_.hx.at[l, 0:32], r_.xe.at[l, R + 32 : R + 64], r_.hx_s.at[0], r_.hx_r.at[l], nodes=prev)
        send(r_.hx.at[l, 32:64], r_.xe.at[l, R : R + 32], r_.hx_s.at[0], r_.hx_r.at[l], nodes=nxt)
        prepare_queries(l)
        for t in range(2, NZ):
            gather_pass(l, t)
        mean0, sq0 = convolution(l)
        sync_start(3 * l, mean0, sq0)
        gather_near(l)
        ready([partner, 2 * z_from(1) + par, 2 * z_from(1) + 1 - par])

        attention_keys(l, 0)
        attention_heads(l, 0, (0, 1))
        gather_far(l)
        ready([2 * z_from(t) + p for t in range(2, NZ) for p in range(2)])
        for i in range(1, NB):
            attention_keys(l, i)
            attention_heads(l, i, (0, 1))
        mean1, sq1 = attention_end(l)
        sync_start(3 * l + 1, mean1, sq1)
        mean0, sq0 = sync_moments(3 * l)
        inv0 = lax.rsqrt(sq0 / total + NORM_EPS)
        r_.iv[l, 0:1] = inv0
        z0 = (r_.z0[l] - mean0) * inv0
        r_.z0[l] = z0
        n0 = z0 * r_.gain[l, 0:1] + r_.shift[l, 0:1]
        r_.local[...] = r_.xf[l] + n0 * sigmoid(n0)
        mean1, sq1 = sync_moments(3 * l + 1)
        inv1 = lax.rsqrt(sq1 / total + NORM_EPS)
        r_.iv[l, 1:2] = inv1
        z1 = (r_.z1[l] - mean1) * inv1
        r_.z1[l] = z1
        mix = r_.local[...] + z1 * r_.gain[l, 1:2] + r_.shift[l, 1:2]
        mb = mix.astype(BF16)
        r_.mb[l] = mb
        u = dot(mb, r_.wu[l])
        r_.u[l] = u
        g = (u * sigmoid(u)).astype(BF16)
        r_.g[l] = g
        y = mix + dot(g, r_.wd[l])
        r_.z2[l] = y
        mean = col_sum(y) / R
        cent = y - mean
        k = 3 * l + 2
        sync_start(k, mean, col_sum(cent * cent))

        if l < L - 1:
            r_.gb[l + 1, me] = cent.astype(BF16)
            gather_start(l + 1)

        if l == L - 1:
            dy = r_.cot[...].astype(F32)
            sync_start(3 * L, col_sum(dy), col_sum(dy * cent))

        tot_mean, tot_sq = sync_moments(k)
        inv2 = lax.rsqrt(tot_sq / total + NORM_EPS)
        r_.iv[l, 2:3] = inv2
        z2 = (r_.z2[l] - tot_mean) * inv2
        r_.z2[l] = z2
        gain, shift = r_.gain[l, 2:3], r_.shift[l, 2:3]
        r_.xf[l + 1] = z2 * gain + shift

        if l == L - 1:
            sync_wait(3 * L)
            sums, means = r_.st1[3 * L], r_.st1[k][:, 0:2]
            mean = jnp.mean(means, 0)
            dy_sum = jnp.sum(sums[:, 0:2], 0)
            dy_cent = jnp.sum(sums[:, 2:4] + (means - mean) * sums[:, 0:2], 0)
            dy_sum, dy_cent = unpack(jnp.concatenate([dy_sum, dy_cent], 0))
            r_.gshift[l, 2:3] = dy_sum
            r_.ggain[l, 2:3] = dy_cent * inv2

        for j in range(N):
            tile = r_.st1[k, rep * N + j]
            r_.moff[j, 0:1] = jnp.concatenate([tile[0:1], tile[1:2]], 1) - tot_mean
        r_.move[0:1] = inv2 * gain
        r_.move[1:2] = shift

    for l in range(L):
        forward(l)
    act_copy = pltpu.make_async_copy(r_.xf.at[L], r_.out_act, r_.store.at[0])
    act_copy.start()

    def back_feed_forward(l, k):
        s2, g2 = r_.gshift[l, 2:3], r_.ggain[l, 2:3]
        d3 = r_.gain[l, 2:3] * r_.iv[l, 2:3] * (r_.dy[...] - s2 / total - r_.z2[l] * (g2 / total))
        db = d3.astype(BF16)
        dub = (dot_nt(db, r_.wd[l]) * silu_slope(r_.u[l])).astype(BF16)
        dmix = d3 + dot_nt(dub, r_.wu[l])
        r_.dmix[...] = dmix
        n0 = r_.z0[l] * r_.gain[l, 0:1] + r_.shift[l, 0:1]
        gy0 = dmix * silu_slope(n0)
        sync_start(k, col_sum(dmix), col_sum(dmix * r_.z1[l]))
        sync_start(k + 1, col_sum(gy0), col_sum(gy0 * r_.z0[l]))
        r_.gy0[...] = gy0
        at = put(r_.gs_early, l, 512, dot_tn(r_.mb[l], dub))
        put(r_.gs_early, l, at, dot_tn(r_.g[l], db))
        r_.xeT[...] = r_.xe[l].T
        r_.qT[...] = r_.q[l].T

    def back_norms(l, k):
        s1, g1 = sync_sums(k)
        r_.gshift[l, 1:2] = s1
        r_.ggain[l, 1:2] = g1
        dmix = r_.dmix[...]
        d2 = r_.gain[l, 1:2] * r_.iv[l, 1:2] * (dmix - s1 / total - r_.z1[l] * (g1 / total))
        dab = d2.astype(BF16)
        r_.dxo[...] = dmix + d2
        r_.dob[...] = dot_nt(dab, r_.wo[l]).astype(BF16).astype(F32)
        put(r_.gs_early, l, 0, dot_tn(r_.ob[l], dab))
        r_.gkv[...] = jnp.zeros((2 * D, D), F32)
        r_.dqT[...] = jnp.zeros((D, R), F32)

    def back_half(i):
        t1 = (i + 1) % NB
        half = (zh + t1) % NB
        place = (NB - t1) % NB
        return place, half, slice(place * W, (place + 1) * W)

    def back_heads(l, i, hf):
        place, half, rows = back_half(i)
        if True:
            lanes = lane_half(hf)
            dos = r_.dob[:, lanes] * r_.rb[l, place, :, lanes]
            prod = dos * r_.oraw[l, :, lanes]
            for k in range(HK):
                r_.dom[k * R : (k + 1) * R, 0:128] = jnp.where(lane_head == k, dos, 0.0).astype(BF16)
                r_.dom[k * R : (k + 1) * R, 128:256] = jnp.where(lane_head == k, -prod, 0.0).astype(BF16)
            r_.dosT[...] = dos.T.astype(BF16)
            values = slice(D + hf * 128, D + (hf + 1) * 128)
            right = jnp.concatenate([r_.kvT[l, values, rows], jnp.ones((128, W), BF16)], 0)
            for c in range(HK // 2):
                both = slice(2 * c * R, 2 * (c + 1) * R)
                r_.sc[c % 2, 0 : 2 * R] = dot(r_.dom[both], right)
                for k in range(2):
                    for at in range(0, R, STRIP):
                        first = (hf * HK + 2 * c + k) * R + at
                        e = r_.pst[l, first : first + STRIP, rows].astype(F32)
                        ds = e * r_.sc[c % 2, k * R + at : k * R + at + STRIP]
                        r_.dss[(2 * c + k) * R + at : (2 * c + k) * R + at + STRIP] = ds.astype(BF16)
                for k in range(2):
                    h = 2 * c + k
                    mine, dims = slice(h * R, (h + 1) * R), head_dims(hf, h)
                    r_.dqT[dims] += dot_nt(r_.kvT[l, dims, rows], r_.dss[mine])
                    r_.dkv[dims] = (dot(r_.qT[dims], r_.dss[mine]) * scale).astype(BF16)
                    dv = dot(r_.dosT[h * HEAD_DIM : (h + 1) * HEAD_DIM], r_.pst[l, head_rows(hf, h), rows])
                    r_.dkv[head_dims(hf, h, D)] = dv.astype(BF16)

    def back_rows(l, i):
        _, half, _ = back_half(i)
        dx = dot(r_.wqkv[l, :, D:], r_.dkv[...]).T
        r_.dxs[l, pl.ds(2 * half, 2)] = dx.astype(BF16).reshape(2, 2, R, D)

        if i < NB - 1:
            for t in (2 * (i + 1), 2 * (i + 1) + 1):
                zb = z_to(t)
                send_rows(r_.dxs.at[l, zb, 1 - par], r_.rs1.at[l, zb], R,
                          r_.rs_s.at[0], r_.rsp_r.at[l, i, t % 2], nodes=partner)

        else:
            near = z_to(1)
            send_rows(r_.dxs.at[l, z, 1 - par], r_.ro.at[l, 0], R, r_.rs_s.at[0], r_.ro_r.at[l], nodes=partner)
            send_rows(r_.dxs.at[l, near, par], r_.ro.at[l, 1], R, r_.rs_s.at[0], r_.ro_r.at[l], nodes=2 * near + par)
            send_rows(r_.dxs.at[l, near, 1 - par], r_.ro.at[l, 2], R, r_.rs_s.at[0], r_.ro_r.at[l],
                 nodes=2 * near + 1 - par)

        r_.gkv[...] += dot(r_.dkv[...], r_.xs[l, pl.ds(4 * half, 4)].reshape(W, D))

    def pass_on(l, i, t):
        zb = z_to(t)
        arrive(r_.rs1.at[l, zb], r_.rsp_r.at[l, i, t % 2])
        both = r_.dxs[l, zb, par].astype(F32) + r_.rs1[l, zb].astype(F32)
        r_.cs[l, zb] = both.astype(BF16)
        send_rows(r_.cs.at[l, zb], r_.rs2.at[l, z], R, r_.rs_s.at[0], r_.rsc_r.at[l], nodes=2 * zb + par)

    def back_convolution(l, k):
        s0, g0 = unpack(jnp.sum(r_.st1[k + 1], 0))
        r_.gshift[l, 0:1] = s0
        r_.ggain[l, 0:1] = g0
        inv_den = 1.0 / (r_.den[l] + GATE_EPS)
        dm = r_.gain[l, 0:1] * r_.iv[l, 0:1] * (r_.gy0[...] - s0 / total - r_.z0[l] * (g0 / total))
        dnum = dm * inv_den
        dden = -dnum * r_.num[l] * inv_den
        high, low = split(jnp.concatenate([dnum, dden], 1))
        r_.dn[0:R] = high
        r_.dn[256 : 256 + R] = low
        r_.sc[0, 0:E, 0 : 2 * D] = dot(r_.le[:, 512:1024], r_.dn[...])
        for at in range(0, E, 64):
            here = slice(at, at + 64)
            gate, dnum_e = r_.gate[l, here], r_.sc[0, here, 0:D]
            dgp = (dnum_e * r_.bs[l, here].astype(F32) + r_.sc[0, here, D : 2 * D]) * gate * (1.0 - gate)
            r_.gg[here, 0:D] = (dnum_e * gate).astype(BF16)
            r_.gg[here, D:] = dgp.astype(BF16)
        ext = dot(r_.ST[...], r_.gg[0:E]).astype(BF16)
        r_.dproj[0:R, 0:D] = dm.astype(BF16)
        r_.dproj[:, D : 2 * D] = ext[:, 0:D]
        r_.dproj[0:R, 2 * D : 3 * D] = dot(r_.TT[:, 0:E], r_.gg[0:E, D:]).astype(BF16)
        r_.dproj[:, 3 * D :] = ext[:, D:]
        dxe = dot_nt(r_.dproj[...], r_.wp[l])
        r_.hs[l, 0] = dxe[R : R + 32].astype(BF16)
        r_.hs[l, 1] = dxe[R + 32 : R + 64].astype(BF16)
        r_.dxo[...] += dxe[0:R]

    def send_halo(l):
        send(r_.hs.at[l, 0], r_.hr.at[l, 1], r_.hal_s.at[0], r_.hal_r.at[l], nodes=prev)
        send(r_.hs.at[l, 1], r_.hr.at[l, 0], r_.hal_s.at[0], r_.hal_r.at[l], nodes=nxt)

    def conv_weight_grads(l):
        at = put(r_.gs_conv, l, 0, dot(r_.xeT[...], r_.dproj[...]))
        put(r_.gs_conv, l, at, dot(r_.efT[...], r_.gg[0:E, D:]))

    def back_input(l):
        dx = r_.dxo[...]
        dx = dx + r_.dxs[l, z, par].astype(F32)
        arrive(r_.ro.at[l], r_.ro_r.at[l])
        for slot in range(3):
            dx = dx + r_.ro[l, slot].astype(F32)
        if NZ > 2:
            arrive(r_.rs2.at[l, 0 : NZ - 2], r_.rsc_r.at[l])
        for t in range(2, NZ):
            dx = dx + r_.rs2[l, z_from(t)].astype(F32)
        arrive(r_.hr.at[l], r_.hal_r.at[l])
        back = jnp.concatenate(
            [r_.hr[l, 0].astype(F32)[0:24], r_.hr[l, 1].astype(F32)[0:24], jnp.zeros((16, D), F32)], 0
        )
        return dx + dot(r_.A[...], back.astype(BF16))

    r_.dy[...] = r_.cot[...].astype(F32)

    E1, C1, Q1, E0, C0, QK0, V0 = range(len(GROUPS))

    def steps(*pairs):
        return [functools.partial(reduce_step, g, k) for g, k in pairs]

    r_.dy[...] = r_.cot[...].astype(F32)

    def backward(b):
        l = L - 1 - b
        first, last = b == 0, b == L - 1
        k = 3 * L + 1 + 2 * b
        back_feed_forward(l, k)
        when(last, *steps((E1, 4), (C1, 3), (Q1, 2)))
        back_norms(l, k)
        if first:
            when(True, *steps((E1, 0)))
            back_heads(l, 0, 0)
            back_heads(l, 0, 1)
            back_rows(l, 0)
            when(True, *steps((E1, 1)))
            back_heads(l, 1, 0)
            pass_on(l, 0, 2)
            back_heads(l, 1, 1)
            back_rows(l, 1)
            pass_on(l, 0, 3)
            sync_wait(k + 1)
            back_convolution(l, k)
            send_halo(l)
            conv_weight_grads(l)
            when(True, *steps((C1, 0)))
        else:
            when(True, *steps((E1, 5), (C1, 4), (Q1, 3), (E0, 0)))
            sync_wait(k + 1)
            back_convolution(l, k)
            send_halo(l)
            when(True, *steps((E0, 1)))
            conv_weight_grads(l)
            when(True, *steps((C0, 0), (E1, 6), (C1, 5), (Q1, 4)))
            back_heads(l, 0, 0)
            when(True, *steps((E0, 2), (C0, 1)))
            back_heads(l, 0, 1)
            back_rows(l, 0)
            when(True, *steps((E0, 3), (C0, 2), (E1, 7), (C1, 6), (Q1, 5)))
            back_heads(l, 1, 0)
            when(True, *steps((E0, 4), (C0, 3), (E1, 8), (C1, 7), (Q1, 6)))
            for t in range(2, NZ):
                pass_on(l, 0, t)
            back_heads(l, 1, 1)
            back_rows(l, 1)
            when(True, *steps((E0, 5), (C0, 4), (C1, 8), (Q1, 7)))
        dqb = (r_.dqT[...].T * scale).astype(BF16)
        r_.dxo[...] += dot_nt(dqb, r_.wqkv[l, :, 0:D])
        at = put(r_.gs_qkv, l, 0, dot(r_.xeT[:, 0:R], dqb))
        put(r_.gs_qkv, l, at, r_.gkv[...].T)
        if first:
            when(True, *steps((Q1, 0), (C1, 1)))
            dx = back_input(l)
            r_.dy[...] = dx
            below = L - 2
            sync_start(SYNCS - 1, col_sum(dx), col_sum(dx * r_.z2[below]))
            when(True, *steps((E1, 2), (Q1, 1)))
            s2, g2 = sync_sums(SYNCS - 1)
            r_.gshift[below, 2:3] = s2
            r_.ggain[below, 2:3] = g2
            when(True, *steps((E1, 3), (C1, 2)))

    for b in range(L):
        backward(b)
    for step in steps((QK0, 0), (V0, 0), (E0, 6), (C0, 5), (Q1, 8), (V0, 1), (QK0, 1)):
        step()
    r_.dy[...] = back_input(0)
    in_copy = pltpu.make_async_copy(r_.dy, r_.grad_in, r_.store.at[1])
    in_copy.start()
    for step in steps(
        (C0, 6), (E0, 7), (V0, 2), (QK0, 2),
        (C0, 7), (E0, 8), (V0, 3), (QK0, 3),
        (C0, 8), (V0, 4), (QK0, 4),
    ):
        step()
    for l in range(L):
        for k in range(3):
            r_.ggain_out[k, l : l + 1] = r_.ggain[l, k : k + 1]
            r_.gshift_out[k, l : l + 1] = r_.gshift[l, k : k + 1]
    for g in range(len(GROUPS)):
        reduce_drain(g)
    sent(r_.meta.at[0 : N - 1], r_.meta_s.at[0])
    sent(r_.st1.at[:, 0 : M * N - 1], r_.st_s.at[0])
    sent(r_.gb.at[:, 0 : 3 + 2 * (NZ - 2)], r_.ag_s.at[0])
    sent(r_.gb.at[:, 0 : 2 * (NB - 1) + 3 + NZ - 2], r_.rs_s.at[0])
    sent(r_.hs, r_.hal_s.at[0])
    sent(r_.hx, r_.hx_s.at[0])
    act_copy.wait()
    in_copy.wait()


def finish_kernel(act_h, gin_h, *refs):
    n = len(GROUPS)
    held, (ggain_h, gshift_h), refs = refs[:n], refs[n : n + 2], refs[n + 2 :]
    act_o, gin_o, proj_o, edge_o, qkv_o, out_o, up_o, down_o, ggain_o, gshift_o = refs[:10]
    summed, refs = refs[10 : 10 + n], refs[10 + n :]
    act, gin, proj, edge, qkv, out, up, down, in_sem, out_sem = refs
    loads = [
        pltpu.make_async_copy(src, dst, in_sem.at[i])
        for i, (src, dst) in enumerate(zip(held + (act_h, gin_h), summed + (act, gin), strict=True))
    ]
    for load in loads:
        load.start()
    ggain_o[...] = ggain_h[...]
    gshift_o[...] = gshift_h[...]
    stores = []

    def store(src, dst):
        copy = pltpu.make_async_copy(src, dst, out_sem.at[len(stores)])
        copy.start()
        stores.append(copy)

    def widen(dst, l, g, at, first=0, last=None):
        rows = dst.shape[1]
        for c in range(first, dst.shape[2] // 128 if last is None else last):
            dst[l, :, 128 * c : 128 * (c + 1)] = summed[g][at : at + rows].astype(F32)
            at += rows
        return at

    for g, (name, l, first, rows, _) in enumerate(GROUPS):
        loads[g].wait()
        if name == "early":
            at = widen(out, l, g, 0)
            store(out.at[l], out_o.at[l])
            at = widen(up, l, g, at)
            store(up.at[l], up_o.at[l])
            widen(down, l, g, at)
            store(down.at[l], down_o.at[l])
        elif name == "conv":
            at = widen(proj, l, g, 0)
            store(proj.at[l], proj_o.at[l])
            widen(edge, l, g, at)
            store(edge.at[l], edge_o.at[l])
        else:
            widen(qkv, l, g, 0, first // 256, (first + rows) // 256)
            if first + rows == 1536:
                store(qkv.at[l], qkv_o.at[l])
    for i, (src, dst) in enumerate(((act, act_o), (gin, gin_o))):
        loads[n + i].wait()
        store(src, dst)
    for copy in stores:
        copy.wait()


def fused_device(
    N, M, node_input, edge_feat, graph_ids, edge_src, edge_dst, halo_send, w_proj, w_edge, w_qkv,
    w_out, w_up, w_down, norm_gain, norm_shift, cotangent,
):
    R, D = node_input.shape
    E = edge_feat.shape[0]
    L = w_proj.shape[0]
    names = scratch_list(N, M, L, R, E)
    vmem = pl.BlockSpec(memory_space=pltpu.VMEM)
    hbm = pl.BlockSpec(memory_space=pltpu.HBM)
    shape = jax.ShapeDtypeStruct
    rows = shape((R, D), F32)
    norm = shape((3, L, D), F32)
    groups = [shape((rows_g, 128), BF16) for _, _, _, rows_g, _ in GROUPS]
    outs = pl.pallas_call(
        functools.partial(kernel, N, M, L, tuple(names)),
        out_shape=[rows, rows, *groups, norm, norm],
        in_specs=[hbm] + [vmem] * 4 + [hbm] * 7 + [vmem] * 2 + [hbm],
        out_specs=[hbm] * (2 + len(GROUPS)) + [vmem] * 2,
        scratch_shapes=list(names.values()),
        compiler_params=pltpu.CompilerParams(
            collective_id=0, has_side_effects=True, vmem_limit_bytes=60 << 20
        ),
        name="layers",
    )(node_input, graph_ids, edge_src, edge_dst, halo_send, edge_feat, w_proj, w_edge, w_qkv, w_out, w_up,
      w_down, norm_gain.transpose(1, 0, 2), norm_shift.transpose(1, 0, 2), cotangent)
    weights = [shape(w.shape, F32) for w in (w_proj, w_edge, w_qkv, w_out, w_up, w_down)]
    results = pl.pallas_call(
        finish_kernel,
        out_shape=[rows, rows, *weights, norm, norm],
        in_specs=[hbm] * (2 + len(GROUPS)) + [vmem] * 2,
        out_specs=[hbm] * 8 + [vmem] * 2,
        scratch_shapes=[pltpu.VMEM(s.shape, s.dtype) for s in (*groups, rows, rows, *weights)]
        + [pltpu.SemaphoreType.DMA((len(GROUPS) + 2,)), pltpu.SemaphoreType.DMA((14,))],
        compiler_params=pltpu.CompilerParams(vmem_limit_bytes=60 << 20),
        name="gradients",
    )(*outs)
    ggain, gshift = results[8].transpose(1, 0, 2), results[9].transpose(1, 0, 2)
    return (*results[:8], ggain, gshift)


BLOCK_CAP = 2048


def extended_2(block, sides, width):
    for axis, dim in sides:
        count = lax.axis_size(axis)
        forward = [(i, i + 1) for i in range(count - 1)]
        forward.append((count - 1, 0))
        backward = [(target, source) for source, target in forward]
        low = lax.ppermute(
            lax.slice_in_dim(block, block.shape[dim] - width, None, axis=dim), axis, forward
        )
        high = lax.ppermute(lax.slice_in_dim(block, 0, width, axis=dim), axis, backward)
        block = jnp.concatenate([low, block, high], axis=dim)
    return block


def block_length(total_rows, upper_limit):
    for length in range(min(total_rows, upper_limit), 0, -1):
        if total_rows % length == 0:
            return length
    return 1


def outer_product(left, right):
    return lax.dot_general(
        left, right, (((0,), (0,)), ((), ())), preferred_element_type=jnp.float32
    )


def times_transposed(left, weight):
    return lax.dot_general(
        left, weight, (((1,), (1,)), ((), ())), preferred_element_type=jnp.float32
    )


def forward_product(left, weight):
    return jnp.dot(left, weight, preferred_element_type=jnp.float32)


def silu_slope_plain(inputs):
    logistic = jax.nn.sigmoid(inputs)
    return logistic * (1.0 + inputs * (1.0 - logistic))


def normalize(inputs, gain_row, shift_row, node_total):
    batch_mean = lax.psum(jnp.sum(inputs, 0), ("nodes", "rep")) / node_total
    centred = inputs - batch_mean
    batch_var = lax.psum(jnp.sum(centred * centred, 0), ("nodes", "rep")) / node_total
    inv_std = lax.rsqrt(batch_var + NORM_EPS)
    standard = (inputs - batch_mean) * inv_std
    return (standard * gain_row + shift_row, standard, inv_std)


def normalize_back(grad_out, standard, inv_std, gain_row, node_total):
    shift_grad, gain_grad = lax.psum(
        (jnp.sum(grad_out, 0), jnp.sum(grad_out * standard, 0)), ("nodes", "rep")
    )
    grad_in = (
        gain_row
        * inv_std
        * (grad_out - shift_grad / node_total - standard * gain_grad / node_total)
    )
    return (grad_in, gain_grad, shift_grad)


def exchange_sources(outgoing):
    halo_rows = outgoing.shape[0] // 2
    grown = extended_2(outgoing, (("nodes", 0),), halo_rows)
    return jnp.concatenate([grown[:halo_rows], grown[3 * halo_rows :]], 0)


def return_sources(incoming_grad):
    halo_rows = incoming_grad.shape[0] // 2
    grown = extended_2(incoming_grad.astype(jnp.bfloat16), (("nodes", 0),), halo_rows).astype(
        incoming_grad.dtype
    )
    return jnp.concatenate([grown[:halo_rows], grown[3 * halo_rows :]], 0)


def attend_forward(query_rows, key_rows, value_rows, local_graphs, group_graphs):
    row_count = query_rows.shape[0]
    score_scale = HEAD_DIM ** (-0.5)
    queries = query_rows.reshape(row_count, HEADS, HEAD_DIM)

    def add_piece(carried, kv_piece, first_row):
        key_piece, value_piece = kv_piece
        piece_rows = key_piece.shape[0]
        block_len = block_length(piece_rows, BLOCK_CAP)

        def add_block(block_state, block_index):
            row_max, row_sum, accumulated = block_state
            block_start = block_index * block_len
            key_block = lax.dynamic_slice_in_dim(key_piece, block_start, block_len, 0).reshape(
                block_len, HEADS, HEAD_DIM
            )
            value_block = lax.dynamic_slice_in_dim(value_piece, block_start, block_len, 0).reshape(
                block_len, HEADS, HEAD_DIM
            )
            key_graphs = lax.dynamic_slice_in_dim(
                group_graphs, first_row + block_start, block_len, 0
            )
            same_graph = (local_graphs[:, None] == key_graphs[None, :])[None]
            scores = (
                jnp.einsum("qhd,khd->hqk", queries, key_block, preferred_element_type=jnp.float32)
                * score_scale
            )
            scores = jnp.where(same_graph, scores, NEG)
            new_max = jnp.maximum(row_max, jnp.max(scores, 2))
            weights = jnp.where(same_graph, jnp.exp(scores - new_max[:, :, None]), 0.0)
            factor = jnp.exp(row_max - new_max)
            row_sum = row_sum * factor + jnp.sum(weights, 2)
            contrib = jnp.einsum(
                "hqk,khd->qhd",
                weights.astype(jnp.bfloat16),
                value_block,
                preferred_element_type=jnp.float32,
            )
            accumulated = accumulated * jnp.transpose(factor)[:, :, None] + contrib
            return ((new_max, row_sum, accumulated), None)

        carried, _ = lax.scan(add_block, carried, jnp.arange(piece_rows // block_len))
        return carried

    start_state = (
        jnp.full((HEADS, row_count), NEG, jnp.float32),
        jnp.zeros((HEADS, row_count), jnp.float32),
        jnp.zeros((row_count, HEADS, HEAD_DIM), jnp.float32),
    )
    row_max, row_sum, accumulated = add_piece(
        start_state,
        (
            lax.all_gather(key_rows, "nodes", axis=0, tiled=True),
            lax.all_gather(value_rows, "nodes", axis=0, tiled=True),
        ),
        jnp.int32(0),
    )
    attn_raw = accumulated / jnp.transpose(row_sum)[:, :, None]
    log_sum = row_max + jnp.log(row_sum)
    return (attn_raw, log_sum)


def attend_backward(
    query_rows, key_rows, value_rows, grad_low, attn_raw, log_sum, local_graphs, group_graphs
):
    row_count = query_rows.shape[0]
    model_width = HEADS * HEAD_DIM
    score_scale = HEAD_DIM ** (-0.5)
    queries = query_rows.reshape(row_count, HEADS, HEAD_DIM)
    grad_heads = grad_low.reshape(row_count, HEADS, HEAD_DIM)
    row_delta = jnp.einsum("qhd,qhd->hq", grad_heads.astype(jnp.float32), attn_raw)

    def score_block(key_block, value_block, key_graphs):
        same_graph = (local_graphs[:, None] == key_graphs[None, :])[None]
        scores = (
            jnp.einsum("qhd,khd->hqk", queries, key_block, preferred_element_type=jnp.float32)
            * score_scale
        )
        attn_weights = jnp.exp(jnp.where(same_graph, scores - log_sum[:, :, None], NEG))
        grad_weights = jnp.einsum(
            "qhd,khd->hqk", grad_heads, value_block, preferred_element_type=jnp.float32
        )
        grad_scores = (attn_weights * (grad_weights - row_delta[:, :, None])).astype(jnp.bfloat16)
        return (attn_weights, grad_scores)

    def key_terms(attn_weights, grad_scores, block_len):
        grad_keys = (
            jnp.einsum("hqk,qhd->khd", grad_scores, queries, preferred_element_type=jnp.float32)
            * score_scale
        )
        grad_values = jnp.einsum(
            "hqk,qhd->khd",
            attn_weights.astype(jnp.bfloat16),
            grad_heads,
            preferred_element_type=jnp.float32,
        )
        return jnp.concatenate(
            [
                grad_keys.reshape(block_len, model_width),
                grad_values.reshape(block_len, model_width),
            ],
            1,
        )

    def query_term(grad_scores, key_block):
        return (
            jnp.einsum("hqk,khd->qhd", grad_scores, key_block, preferred_element_type=jnp.float32)
            * score_scale
        )

    group_rows = group_graphs.shape[0]

    def add_piece(carried, kv_piece, first_row):
        key_piece, value_piece = kv_piece
        piece_rows = key_piece.shape[0]
        block_len = block_length(piece_rows, BLOCK_CAP)

        def add_block(block_state, block_index):
            grad_query, buffer = block_state
            block_start = block_index * block_len
            key_block = lax.dynamic_slice_in_dim(key_piece, block_start, block_len, 0).reshape(
                block_len, HEADS, HEAD_DIM
            )
            value_block = lax.dynamic_slice_in_dim(value_piece, block_start, block_len, 0).reshape(
                block_len, HEADS, HEAD_DIM
            )
            place = first_row + block_start
            key_graphs = lax.dynamic_slice_in_dim(group_graphs, place, block_len, 0)
            attn_weights, grad_scores = score_block(key_block, value_block, key_graphs)
            grad_query = grad_query + query_term(grad_scores, key_block)
            block_terms = key_terms(attn_weights, grad_scores, block_len)
            current = lax.dynamic_slice_in_dim(buffer, place, block_len, 0)
            buffer = lax.dynamic_update_slice_in_dim(buffer, current + block_terms, place, 0)
            return ((grad_query, buffer), None)

        carried, _ = lax.scan(add_block, carried, jnp.arange(piece_rows // block_len))
        return carried

    start_state = (
        jnp.zeros((row_count, HEADS, HEAD_DIM), jnp.float32),
        jnp.zeros((group_rows, 2 * model_width), jnp.float32),
    )
    grad_query, buffer = add_piece(
        start_state,
        (
            lax.all_gather(key_rows, "nodes", axis=0, tiled=True),
            lax.all_gather(value_rows, "nodes", axis=0, tiled=True),
        ),
        jnp.int32(0),
    )
    grad_kv = lax.psum_scatter(buffer, "nodes", scatter_dimension=0, tiled=True)
    return (
        grad_query.reshape(row_count, model_width),
        grad_kv[:, :model_width],
        grad_kv[:, model_width:],
    )


def layer_forward(
    hidden, params, edge_feat, edge_src, edge_dst, halo_send, local_graphs, group_graphs, node_total
):
    w_proj, w_edge, w_qkv, w_out, w_up, w_down, norm_gains, norm_shifts = params
    row_count, model_width = hidden.shape
    hidden_low = hidden.astype(jnp.bfloat16)
    projected = forward_product(hidden_low, w_proj)
    self_term = projected[:, :model_width]
    dest_term = projected[:, 2 * model_width : 3 * model_width]
    source_rows = jnp.concatenate(
        [projected[:, model_width : 2 * model_width], projected[:, 3 * model_width :]], 1
    ).astype(jnp.bfloat16)
    incoming = exchange_sources(source_rows[halo_send])
    extended = jnp.concatenate([source_rows, incoming], 0)
    edge_rows = extended[edge_src].astype(jnp.float32)
    source_b = edge_rows[:, :model_width]
    source_e = edge_rows[:, model_width:]
    edge_proj = forward_product(edge_feat, w_edge)
    gating = jax.nn.sigmoid(dest_term[edge_dst] + source_e + edge_proj)
    numerator = jax.ops.segment_sum(gating * source_b, edge_dst, row_count)
    denominator = jax.ops.segment_sum(gating, edge_dst, row_count)
    message = self_term + numerator / (denominator + GATE_EPS)
    normed_one, standard_one, inv_one = normalize(
        message, norm_gains[0], norm_shifts[0], node_total
    )
    local_out = hidden + jax.nn.silu(normed_one)
    qkv_low = forward_product(hidden_low, w_qkv).astype(jnp.bfloat16)
    query_rows = qkv_low[:, :model_width]
    key_rows = qkv_low[:, model_width : 2 * model_width]
    value_rows = qkv_low[:, 2 * model_width :]
    attn_raw, log_sum = attend_forward(query_rows, key_rows, value_rows, local_graphs, group_graphs)
    attn_low = attn_raw.reshape(row_count, model_width).astype(jnp.bfloat16)
    attn_proj = forward_product(attn_low, w_out)
    normed_two, standard_two, inv_two = normalize(
        hidden + attn_proj, norm_gains[1], norm_shifts[1], node_total
    )
    mixed = local_out + normed_two
    mixed_low = mixed.astype(jnp.bfloat16)
    up_proj = forward_product(mixed_low, w_up)
    activated = jax.nn.silu(up_proj).astype(jnp.bfloat16)
    down_proj = forward_product(activated, w_down)
    normed_three, standard_three, inv_three = normalize(
        mixed + down_proj, norm_gains[2], norm_shifts[2], node_total
    )
    saved = (
        hidden_low,
        source_b,
        gating,
        numerator,
        denominator,
        normed_one,
        standard_one,
        inv_one,
        query_rows,
        key_rows,
        value_rows,
        attn_raw,
        log_sum,
        attn_low,
        standard_two,
        inv_two,
        mixed_low,
        up_proj,
        activated,
        standard_three,
        inv_three,
    )
    return (normed_three, saved)


def layer_backward(
    grad_out,
    params,
    saved,
    edge_feat,
    edge_src,
    edge_dst,
    halo_send,
    local_graphs,
    group_graphs,
    node_total,
):
    w_proj, w_edge, w_qkv, w_out, w_up, w_down, norm_gains, norm_shifts = params
    (
        hidden_low,
        source_b,
        gating,
        numerator,
        denominator,
        normed_one,
        standard_one,
        inv_one,
        query_rows,
        key_rows,
        value_rows,
        attn_raw,
        log_sum,
        attn_low,
        standard_two,
        inv_two,
        mixed_low,
        up_proj,
        activated,
        standard_three,
        inv_three,
    ) = saved
    row_count, model_width = grad_out.shape
    grad_three, gain_three, shift_three = normalize_back(
        grad_out, standard_three, inv_three, norm_gains[2], node_total
    )
    down_grad = grad_three.astype(jnp.bfloat16)
    grad_w_down = outer_product(activated, down_grad)
    up_grad = (times_transposed(down_grad, w_down) * silu_slope_plain(up_proj)).astype(jnp.bfloat16)
    grad_w_up = outer_product(mixed_low, up_grad)
    grad_mixed = grad_three + times_transposed(up_grad, w_up)
    grad_two, gain_two, shift_two = normalize_back(
        grad_mixed, standard_two, inv_two, norm_gains[1], node_total
    )
    out_grad = grad_two.astype(jnp.bfloat16)
    grad_w_out = outer_product(attn_low, out_grad)
    attn_grad = times_transposed(out_grad, w_out).astype(jnp.bfloat16)
    grad_query, grad_key, grad_value = attend_backward(
        query_rows, key_rows, value_rows, attn_grad, attn_raw, log_sum, local_graphs, group_graphs
    )
    qkv_grad = jnp.concatenate([grad_query, grad_key, grad_value], 1).astype(jnp.bfloat16)
    grad_w_qkv = outer_product(hidden_low, qkv_grad)
    grad_message, gain_one, shift_one = normalize_back(
        grad_mixed * silu_slope_plain(normed_one), standard_one, inv_one, norm_gains[0], node_total
    )
    shifted = denominator + GATE_EPS
    grad_numer = grad_message / shifted
    grad_denom = -grad_message * numerator / (shifted * shifted)
    numer_edge = grad_numer[edge_dst]
    grad_gate = numer_edge * source_b + grad_denom[edge_dst]
    grad_pre_edge = grad_gate * gating * (1.0 - gating)
    edge_grad = grad_pre_edge.astype(jnp.bfloat16)
    grad_w_edge = outer_product(edge_feat, edge_grad)
    grad_dest = jax.ops.segment_sum(grad_pre_edge, edge_dst, row_count)
    grad_extended = jax.ops.segment_sum(
        jnp.concatenate([numer_edge * gating, grad_pre_edge], 1),
        edge_src,
        row_count + halo_send.shape[0],
    )
    returned = return_sources(grad_extended[row_count:])
    grad_source = grad_extended[:row_count].at[halo_send].add(returned)
    proj_grad = jnp.concatenate(
        [grad_message, grad_source[:, :model_width], grad_dest, grad_source[:, model_width:]], 1
    ).astype(jnp.bfloat16)
    grad_w_proj = outer_product(hidden_low, proj_grad)
    grad_hidden = (
        grad_mixed
        + grad_two
        + times_transposed(proj_grad, w_proj)
        + times_transposed(qkv_grad, w_qkv)
    )
    weight_grads = (grad_w_proj, grad_w_edge, grad_w_qkv, grad_w_out, grad_w_up, grad_w_down)
    return (
        grad_hidden,
        weight_grads,
        jnp.stack([gain_one, gain_two, gain_three]),
        jnp.stack([shift_one, shift_two, shift_three]),
    )


def per_device(
    node_input,
    edge_feat,
    graph_ids,
    edge_src,
    edge_dst,
    halo_send,
    w_proj,
    w_edge,
    w_qkv,
    w_out,
    w_up,
    w_down,
    norm_gain,
    norm_shift,
    cotangent,
):
    group_graphs = lax.all_gather(graph_ids, "nodes", axis=0, tiled=True)
    node_total = node_input.shape[0] * lax.axis_size("nodes") * lax.axis_size("rep")
    layer_count = w_proj.shape[0]
    layer_params = [
        (
            w_proj[layer_index],
            w_edge[layer_index],
            w_qkv[layer_index],
            w_out[layer_index],
            w_up[layer_index],
            w_down[layer_index],
            norm_gain[layer_index],
            norm_shift[layer_index],
        )
        for layer_index in range(layer_count)
    ]
    hidden = node_input.astype(jnp.float32)
    saved_all = []
    for layer_index in range(layer_count):
        hidden, saved = layer_forward(
            hidden,
            layer_params[layer_index],
            edge_feat,
            edge_src,
            edge_dst,
            halo_send,
            graph_ids,
            group_graphs,
            node_total,
        )
        saved_all.append(saved)
    grad_hidden = cotangent.astype(jnp.float32)
    weight_parts = [None] * layer_count
    gain_parts = [None] * layer_count
    shift_parts = [None] * layer_count
    for layer_index in range(layer_count - 1, -1, -1):
        (
            grad_hidden,
            weight_parts[layer_index],
            gain_parts[layer_index],
            shift_parts[layer_index],
        ) = layer_backward(
            grad_hidden,
            layer_params[layer_index],
            saved_all[layer_index],
            edge_feat,
            edge_src,
            edge_dst,
            halo_send,
            graph_ids,
            group_graphs,
            node_total,
        )
    proj_local = jnp.stack([weight_parts[layer_index][0] for layer_index in range(layer_count)])
    edge_local = jnp.stack([weight_parts[layer_index][1] for layer_index in range(layer_count)])
    qkv_local = jnp.stack([weight_parts[layer_index][2] for layer_index in range(layer_count)])
    out_local = jnp.stack([weight_parts[layer_index][3] for layer_index in range(layer_count)])
    up_local = jnp.stack([weight_parts[layer_index][4] for layer_index in range(layer_count)])
    down_local = jnp.stack([weight_parts[layer_index][5] for layer_index in range(layer_count)])
    grad_proj, grad_edge, grad_qkv, grad_out, grad_up, grad_down = lax.psum(
        (proj_local, edge_local, qkv_local, out_local, up_local, down_local), ("nodes", "rep")
    )
    return (
        hidden,
        grad_hidden,
        grad_proj,
        grad_edge,
        grad_qkv,
        grad_out,
        grad_up,
        grad_down,
        jnp.stack(gain_parts),
        jnp.stack(shift_parts),
    )


def solution(mesh):
    in_specs = (
        P(("rep", "nodes"), None),
        P(("rep", "nodes"), None),
        P(("rep", "nodes")),
        P(("rep", "nodes")),
        P(("rep", "nodes")),
        P(("rep", "nodes")),
        P(),
        P(),
        P(),
        P(),
        P(),
        P(),
        P(),
        P(),
        P(("rep", "nodes"), None),
    )
    out_specs = (
        P(("rep", "nodes"), None),
        P(("rep", "nodes"), None),
        P(),
        P(),
        P(),
        P(),
        P(),
        P(),
        P(),
        P(),
    )
    N, M = mesh.shape["nodes"], mesh.shape["rep"]
    fused = N in (4, 8) and M % 2 == 0 and 512 % (16 * N * M) == 0
    return jax.shard_map(
        functools.partial(fused_device, N, M) if fused else per_device,
        mesh=mesh, in_specs=in_specs, out_specs=out_specs, check_vma=False,
    )
```
